32 devices in a mesh: spot: 16 (over z, y, x), gene: 2 (over core).
Axes of the slice: x: 2, y: 2, z: 4, core: 2. Of those that a mesh axis runs over, the one named last changes fastest.
Arguments:
- logits: float32 [2, 1024, 2048], P(None, 'spot'), may hold values from -12 to 12
- expr: float32 [2048, 2048], P('spot', 'gene'), may hold values from -6 to 6
- spatial: float32 [2, 1024, 2048], P(None, 'spot', 'gene')
- slide_spots: int32 [2], replicated, may hold values from 768 to 1024, as said below
- spot_cells: int32 [2, 1024], P(None, 'spot'), may hold values from 1 to 20
- cell_prior: int32 [2048], replicated, may hold values from 4096 to 262143
Outputs:
- pred: float32 [2, 1024, 2048], P(None, 'spot', 'gene')
- loss: float32 [], replicated
- grad_logits: float32 [2, 1024, 2048], P(None, 'spot')
- grad_expr: float32 [2048, 2048], P('spot', 'gene')
The draws below stay inside these ranges and needn't reach their ends.
Inputs may be any that keep to these rules, and one draw needn't show every extreme that they name: `slide_spots`: one slide, drawn from the seed, fills all 1024 slots in every draw; every other slide leaves at least one slot empty.
All inputs are finite; a program needn't handle non-finite values.
Results may differ from the reference program's by a relative error of at most 0.0003.
Values sent between devices are 32-bit elements; how exact they have to be, the bound alone decides.
A program may use at most 192 MiB of HBM per device.

```python
import jax
import jax.numpy as jnp
from jax import lax

GENES = 2048
MB = 2
CELLS = 2048
SPOTS_MB = 1024


def draw_spatial(key, part):
    key = jax.random.fold_in(key, 1)
    first, second, third = jax.random.split(key, 3)
    row_scale = jnp.exp(jax.random.uniform(second, (MB, SPOTS_MB, 1)) * 2.302585) / 3.0
    col_scale = jnp.exp(jax.random.uniform(third, (1, 1, GENES)) * 2.302585) / 3.0
    base = jax.random.normal(first, (MB, SPOTS_MB, GENES))
    return (base * row_scale * col_scale).astype(jnp.float32)


def draw_slide_spots(key, part):
    key = jax.random.fold_in(key, 2)
    first, second = jax.random.split(key)
    shortfall = jax.random.randint(first, (MB,), 1, SPOTS_MB // 4 + 1)
    full_one = jax.random.randint(second, (), 0, MB)
    shortfall = jnp.where(jnp.arange(MB) == full_one, 0, shortfall)
    return (SPOTS_MB - shortfall).astype(jnp.int32)


def plant(drawn, key, least, largest):
    extent = drawn.shape
    spot = [jax.random.randint(jax.random.fold_in(key, axis), (), 0, extent[axis]) for axis in range(len(extent))]
    drawn = drawn.at[tuple(spot)].set(least)
    longest = extent.index(max(extent))
    spot[longest] = (spot[longest] + 1) % extent[longest]
    return drawn.at[tuple(spot)].set(largest)


def level_of(stream_key, extent, cuts, least, high):
    def one(axis_at, parts):
        draws = jax.random.uniform(jax.random.fold_in(jax.random.fold_in(stream_key, 6), axis_at), (parts,), jnp.float32, least / len(cuts), high / len(cuts))
        return jnp.repeat(jnp.exp(draws), extent[axis_at] // parts).reshape((-1,) + (1,) * (len(extent) - axis_at - 1))

    gain = one(*cuts[0])
    for cut in cuts[1:]:
        gain = gain * one(*cut)
    return gain


def gaussian(stream_key, dims, deviation, bound, shards=(), kind=jnp.bfloat16):
    array = jax.random.normal(stream_key, dims, jnp.float32) * deviation
    if len(shards) > 0:
        array = level_of(stream_key, dims, shards, -0.22, 0.18) * array
    return jnp.clip(array, min=-bound, max=bound).astype(kind)


def setup_inputs(seed: int = 0) -> dict:
    arg_keys = jax.random.split(jax.random.key(seed), 7)
    return {
        "logits": gaussian(arg_keys[0], (MB, SPOTS_MB, CELLS), 2.0, 12.0, ((1, 16),), jnp.float32),
        "expr": gaussian(arg_keys[1], (CELLS, GENES), 1.0, 6.0, ((0, 16), (1, 2)), jnp.float32),
        "spatial": draw_spatial(jax.random.fold_in(arg_keys[6], 71), 0),
        "slide_spots": draw_slide_spots(jax.random.fold_in(arg_keys[6], 71), 0),
        "spot_cells": plant(jax.random.randint(arg_keys[4], (MB, SPOTS_MB), 1, 21), jax.random.fold_in(arg_keys[4], 1), 1, 20).astype(jnp.int32),
        "cell_prior": plant(jax.random.randint(arg_keys[5], (CELLS,), 4096, 262144), jax.random.fold_in(arg_keys[5], 1), 4096, 262143).astype(jnp.int32),
    }


@jax.custom_vjp
def low(v):
    return lax.optimization_barrier(v.astype(jnp.bfloat16)).astype(jnp.float32)

@jax.custom_vjp
def low_back(v):
    return v

def low_keep(v):
    return (low(v), None)

def low_pass(kept, grad):
    return (grad,)

def back_keep(v):
    return (v, None)

def back_low(kept, grad):
    return (low(grad),)
low.defvjp(low_keep, low_pass)
low_back.defvjp(back_keep, back_low)
tiny = 1e-06
fixed_point = 16384.0

def slide_terms(logit_m, spatial_m, count_m, cells_m, expr_all, weights):
    probs = jax.nn.softmax(logit_m, axis=1)
    pred = jnp.dot(probs, expr_all, precision=lax.Precision.HIGHEST)
    positions = jnp.arange(logit_m.shape[0], dtype=jnp.int32)
    valid = (positions < count_m).astype(jnp.float32)
    gene_dot = lax.optimization_barrier(jnp.sum(valid[:, None] * pred * spatial_m, axis=0))
    gene_pred = lax.optimization_barrier(jnp.sum(valid[:, None] * pred * pred, axis=0))
    gene_true = lax.optimization_barrier(jnp.sum(valid[:, None] * spatial_m * spatial_m, axis=0))
    cos_gene = gene_dot * lax.rsqrt(gene_pred * gene_true + tiny)
    spot_dot = lax.optimization_barrier(jnp.sum(pred * spatial_m, axis=1))
    spot_pred = lax.optimization_barrier(jnp.sum(pred * pred, axis=1))
    spot_true = lax.optimization_barrier(jnp.sum(spatial_m * spatial_m, axis=1))
    cos_spot = spot_dot * lax.rsqrt(spot_pred * spot_true + tiny)
    mass = jnp.dot(probs, weights, precision=lax.Precision.HIGHEST)
    mass_total = jnp.sum(valid * mass)
    counted = cells_m.astype(jnp.float32)
    kcell = valid * counted
    cell_total = jnp.sum(kcell)
    target = kcell / cell_total
    kl_value = jnp.sum(target * (jnp.log(counted) - jnp.log(cell_total) - jnp.log(mass) + jnp.log(mass_total)))
    loss = -jnp.sum(cos_gene) - jnp.sum(valid * cos_spot) + count_m.astype(jnp.float32) * kl_value
    return (pred, loss)

def reference(logits, expr, spatial, slide_spots, spot_cells, cell_prior):
    weights = cell_prior.astype(jnp.float32) / fixed_point

    def forward(logit_all, expr_all):

        def single(items):
            return slide_terms(items[0], items[1], items[2], items[3], expr_all, weights)
        preds, losses = lax.map(jax.checkpoint(single), (logit_all, spatial, slide_spots, spot_cells))
        return (jnp.sum(losses), preds)
    loss, pullback, preds = jax.vjp(forward, logits, expr, has_aux=True)
    grad_logits, grad_expr = pullback(jnp.ones_like(loss))
    return (preds, loss, grad_logits, grad_expr)
```

```python
import functools

import jax
import jax.numpy as jnp
from jax import lax
from jax.experimental import pallas as pl
from jax.experimental.pallas import tpu as pltpu
from jax.sharding import PartitionSpec as P

tiny = 1e-06
fixed_point = 16384.0
F32 = jnp.float32
BF16 = jnp.bfloat16
MESH = pl.DeviceIdType.MESH

PLANE = 4
LANES = 128
CHUNKS = 4
STEP_ROWS = 16


def halves(value):
    high = value.astype(BF16)
    return high, (value - high.astype(F32)).astype(BF16)


def product(a_high, a_low, b_high, b_low, contract):
    def one(a, b):
        return lax.dot_general(a, b, (contract, ((), ())), preferred_element_type=F32)

    return one(a_high, b_high) + (one(a_high, b_low) + one(a_low, b_high))


def plane_kernel(
    lines,
    chunks,
    logits_ref,
    expr_ref,
    spatial_ref,
    count_ref,
    cells_ref,
    prior_ref,
    pred_ref,
    loss_ref,
    glog_ref,
    gexp_ref,
    lg,
    tg,
    pq,
    ab,
    ahi,
    alo,
    thi,
    tlo,
    bb,
    bhi,
    blo,
    cs,
    cr,
    pr,
    sacc,
    s1,
    s2,
    gv,
    ss,
    rowv,
    ds,
    es,
    ru,
    rd,
    fs,
    fr,
    fo,
    go,
    ge,
    inn,
    l1,
    l2,
    loc,
    exl,
    ag_r,
    ag_us,
    ag_ds,
    a_s,
    a_r,
    c_s,
    c_r,
    s1_s,
    s1_r,
    s2_s,
    s2_r,
    ss_s,
    ss_r,
    d_s,
    d_r,
    ru_s,
    ru_r,
    rd_s,
    rd_r,
    f_s,
    f_r,
    fo_s,
    fo_r,
    in_s,
    in_r,
    l1_s,
    l1_r,
    l2_s,
    l2_r,
    out_s,
):
    place = lax.axis_index("spot")
    core = lax.axis_index("gene")
    z = place // PLANE
    q = place % PLANE
    col, row = q % 2, q // 2
    mates = ((1 - row) * 2 + 1 - col, row * 2 + 1 - col, (1 - row) * 2 + col)
    others = tuple((z + step) % lines for step in range(1, lines))
    up, down = (place + PLANE, core), (place - PLANE, core)
    sibling = (place, 1 - core)
    slides, slide_rows = logits_ref.shape[0], logits_ref.shape[1]
    rows = slides * slide_rows
    cb = expr_ref.shape[0]
    genes = expr_ref.shape[1]
    width = genes // chunks
    last = lines - 1

    def mate(p):
        return (z * PLANE + p, core)

    def send(src, dst, send_sem, recv_sem, device):
        copy = pltpu.make_async_remote_copy(
            src_ref=src, dst_ref=dst, send_sem=send_sem, recv_sem=recv_sem, device_id=device, device_id_type=MESH
        )
        copy.start()

    def arrived(dst, recv_sem):
        pltpu.make_async_copy(dst, dst, recv_sem).wait()

    sent = arrived

    def cols(k):
        return pl.ds(k * width, width)

    def block(index):
        return pl.ds(pl.multiple_of(index * cb, cb), cb)

    def share(index):
        return pl.ds(pl.multiple_of(index * rows, rows), rows)

    for m in range(slides):
        part = pl.ds(m * slide_rows, slide_rows)
        pltpu.make_async_copy(logits_ref.at[m], lg.at[part], loc.at[m]).start()
        pltpu.make_async_copy(spatial_ref.at[m], tg.at[part], loc.at[slides + m]).start()
    for k in range(chunks):
        pltpu.make_async_copy(expr_ref.at[:, cols(k)], bb.at[k, block(z)], exl.at[k]).start()

    barrier = pltpu.get_barrier_semaphore()
    for p in mates:
        pl.semaphore_signal(barrier, inc=1, device_id=mate(p), device_id_type=MESH)
    for o in others:
        pl.semaphore_signal(barrier, inc=1, device_id=(o * PLANE + q, core), device_id_type=MESH)
    pl.semaphore_signal(barrier, inc=1, device_id=sibling, device_id_type=MESH)
    pl.semaphore_wait(barrier, len(mates) + len(others) + 1)

    for k in range(chunks):

        @pl.when(z < last)
        def _():
            send(expr_ref.at[:, cols(k)], bb.at[k, block(z)], ag_us.at[z], ag_r.at[z, k], up)

        @pl.when(z > 0)
        def _():
            send(expr_ref.at[:, cols(k)], bb.at[k, block(z)], ag_ds.at[z], ag_r.at[z, k], down)

    def forward(k, distance):
        below, above = z - distance, z + distance

        @pl.when(below >= 0)
        def _():
            here = bb.at[k, block(below)]
            arrived(here, ag_r.at[below, k])

            @pl.when(z < last)
            def _():
                send(here, here, ag_us.at[below], ag_r.at[below, k], up)

        @pl.when(above <= last)
        def _():
            here = bb.at[k, block(above)]
            arrived(here, ag_r.at[above, k])

            @pl.when(z > 0)
            def _():
                send(here, here, ag_ds.at[above], ag_r.at[above, k], down)

    weights = prior_ref[...].astype(F32) / fixed_point
    for m in range(slides):
        part = pl.ds(m * slide_rows, slide_rows)
        pltpu.make_async_copy(logits_ref.at[m], lg.at[part], loc.at[m]).wait()

    @pl.loop(0, rows // STEP_ROWS)
    def _(step):
        at = pl.ds(pl.multiple_of(step * STEP_ROWS, STEP_ROWS), STEP_ROWS)
        value = lg[at, :]
        raised = jnp.exp(value - jnp.max(value, axis=1, keepdims=True))
        probs = raised / jnp.sum(raised, axis=1, keepdims=True)
        mass_rows = jnp.sum(probs * weights, axis=1, keepdims=True)
        rowv[0, at, :] = jnp.broadcast_to(mass_rows, (STEP_ROWS, LANES))
        for p in range(PLANE):
            for line in range(lines):
                at_cells = (line * PLANE + p) * cb
                pq[p, at, pl.ds(line * cb, cb)] = probs[:, at_cells : at_cells + cb]

    for p in mates:
        send(pq.at[p], ab.at[q], a_s, a_r.at[q], mate(p))
    ab[q] = pq[q]

    rid = lax.broadcasted_iota(jnp.int32, (rows, 1), 0)
    first = rid < slide_rows
    position = place * slide_rows + jnp.where(first, rid, rid - slide_rows)
    count = jnp.where(first, count_ref[0], count_ref[1])
    valid = (position < count).astype(F32)
    scale_count = count.astype(F32)
    square = (slide_rows, slide_rows)
    eye = lax.broadcasted_iota(jnp.int32, square, 0) == lax.broadcasted_iota(jnp.int32, square, 1)
    counted = jnp.concatenate(
        [
            jnp.sum(jnp.where(eye, cells_ref[m : m + 1, :].astype(F32), 0.0), axis=1, keepdims=True)
            for m in range(slides)
        ],
        axis=0,
    )
    mass = rowv[0, :, 0:1]
    kcell = valid * counted

    def by_slide(value):
        return [jnp.sum(value[m * slide_rows : (m + 1) * slide_rows], axis=0, keepdims=True) for m in range(slides)]

    mass_parts = by_slide(valid * mass)
    cell_parts = by_slide(kcell)
    lane = lax.broadcasted_iota(jnp.int32, (1, width), 1)
    scalars = jnp.zeros((1, width), F32)
    for at, value in enumerate(mass_parts + cell_parts):
        scalars = jnp.where(lane == at, value, scalars)

    for m in range(slides):
        part = pl.ds(m * slide_rows, slide_rows)
        pltpu.make_async_copy(spatial_ref.at[m], tg.at[part], loc.at[slides + m]).wait()
    sacc[...] = jnp.zeros_like(sacc)

    for k in range(min(2, chunks)):
        forward(k, 1)

    for p in mates:
        arrived(ab.at[p], a_r.at[p])
    for p in range(PLANE):
        at = pl.ds(p * rows, rows)
        high, low = halves(ab[p])
        ahi[at, :], alo[at, :] = high, low
        high, low = halves(ab[p].T)
        thi[:, at], tlo[:, at] = high, low

    def forward_product(k):
        pltpu.make_async_copy(expr_ref.at[:, cols(k)], bb.at[k, block(z)], exl.at[k]).wait()
        high, low = halves(bb[k])
        bhi[k], blo[k] = high, low
        cs[k] = product(ahi[...], alo[...], high, low, ((1,), (0,)))
        for p in mates:
            send(cs.at[k, share(p)], cr.at[k, q], c_s, c_r.at[k, q], mate(p))

    def finish_pred(k):
        total = cs[k, share(q), :]
        for p in mates:
            arrived(cr.at[k, p], c_r.at[k, p])
            total = total + cr[k, p]
        pr[k] = total
        truth = tg[:, cols(k)]
        for m in range(slides):
            part = pl.ds(m * slide_rows, slide_rows)
            pltpu.make_async_copy(pr.at[k, part], pred_ref.at[m, :, cols(k)], out_s.at[m]).start()
        sacc[0] += total * truth
        sacc[1] += total * total
        sacc[2] += truth * truth
        kept = valid * total
        stats = by_slide(kept * truth) + by_slide(kept * total) + by_slide(valid * truth * truth)
        s1[q, :, cols(k)] = jnp.concatenate(stats + [scalars, jnp.zeros((1, width), F32)], axis=0)

    for k in range(chunks):
        for distance in range(2, lines):
            forward(k, distance)
        if k + 2 < chunks:
            forward(k + 2, 1)
        forward_product(k)
        if k >= 1:
            finish_pred(k - 1)
    finish_pred(chunks - 1)

    for p in mates:
        send(s1.at[q], s1.at[q], s1_s, s1_r.at[q], mate(p))
    wide = lax.broadcasted_iota(jnp.int32, (rows, LANES), 1)
    sums = [jnp.sum(sacc[at], axis=1, keepdims=True) for at in range(3)]
    ss[core] = jnp.where(wide == 0, sums[0], jnp.where(wide == 1, sums[1], sums[2]))
    send(ss.at[core], ss.at[core], ss_s, ss_r, sibling)
    for p in mates:
        arrived(s1.at[p], s1_r.at[p])
    s2[z] = (s1[0] + s1[1]) + (s1[2] + s1[3])
    for o in others:
        send(s2.at[z], s2.at[z], s2_s, s2_r.at[z], (o * PLANE + q, core))
    arrived(ss.at[1 - core], ss_r)
    spot = ss[0] + ss[1]
    spot_dot, spot_pred, spot_true = spot[:, 0:1], spot[:, 1:2], spot[:, 2:3]
    spot_inv = lax.rsqrt(spot_pred * spot_true + tiny)
    cos_spot = spot_dot * spot_inv
    spot_back = cos_spot * spot_true / (spot_pred * spot_true + tiny)
    for o in others:
        arrived(s2.at[o], s2_r.at[o])
    total = s2[0]
    for line in range(1, lines):
        total = total + s2[line]
    gene_dot, gene_pred, gene_true = total[0:2], total[2:4], total[4:6]
    gene_inv = lax.rsqrt(gene_pred * gene_true + tiny)
    cos_gene = gene_dot * gene_inv
    gv[0:2, :] = gene_inv
    gv[2:4, :] = cos_gene * gene_true / (gene_pred * gene_true + tiny)

    inner = jnp.zeros((rows, 1), F32)
    for k in range(chunks):
        parts = []
        for m in range(slides):
            lo, hi = m * slide_rows, (m + 1) * slide_rows
            truth, guess = tg[lo:hi, cols(k)], pr[k, lo:hi, :]
            inverse, back = gv[m : m + 1, cols(k)], gv[2 + m : 3 + m, cols(k)]
            parts.append(
                -valid[lo:hi]
                * (truth * (inverse + spot_inv[lo:hi]) - guess * back - guess * spot_back[lo:hi])
            )
        grad = jnp.concatenate(parts, axis=0)
        ds[k, q] = grad
        for p in mates:
            send(ds.at[k, q], ds.at[k, q], d_s, d_r.at[k, q], mate(p))
        inner = inner + jnp.sum(grad * pr[k], axis=1, keepdims=True)
    gene_sum = jnp.sum(jnp.sum(cos_gene, axis=1, keepdims=True), axis=0, keepdims=True)
    inn[core] = jnp.where(wide == 0, inner, gene_sum)
    send(inn.at[core], inn.at[core], in_s, in_r, sibling)

    mass_total = jnp.where(first, total[6:7, 0:1], total[6:7, 1:2])
    cell_total = jnp.where(first, total[6:7, 2:3], total[6:7, 3:4])
    portion = kcell / cell_total
    kl_rows = portion * (jnp.log(counted) - jnp.log(cell_total) - jnp.log(mass) + jnp.log(mass_total))
    dmass = scale_count * valid * (1.0 / mass_total - portion / mass)
    terms = jnp.sum(scale_count * kl_rows - valid * cos_spot, axis=0, keepdims=True)
    l1[q] = jnp.broadcast_to(terms, (8, LANES))
    for p in mates:
        send(l1.at[q], l1.at[q], l1_s, l1_r.at[q], mate(p))

    def backward_product(k):
        for p in mates:
            arrived(ds.at[k, p], d_r.at[k, p])
        high, low = halves(ds[k].reshape(PLANE * rows, width))
        es[k] = product(thi[...], tlo[...], high, low, ((1,), (0,)))

        @pl.when(z == 0)
        def _():
            for line in range(last, 0, -1):
                here = es.at[k, block(line)]
                send(here, ru.at[k, block(line)], ru_s.at[line], ru_r.at[line, k], up)

        @pl.when(z == last)
        def _():
            for line in range(last):
                here = es.at[k, block(line)]
                send(here, rd.at[k, block(line)], rd_s.at[line], rd_r.at[line, k], down)

        part = product(high, low, bhi[k], blo[k], ((1,), (1,)))
        if k == 0:
            fs[...] = part
        else:
            fs[...] += part

    def add_on(k):
        for line in range(last, 1, -1):
            at = block(line)

            @pl.when((z > 0) & (z < line))
            def _():
                arrived(ru.at[k, at], ru_r.at[line, k])
                es[k, at, :] += ru[k, at, :]
                send(es.at[k, at], ru.at[k, at], ru_s.at[line], ru_r.at[line, k], up)

        for line in range(last - 1):
            at = block(line)

            @pl.when((z < last) & (z > line))
            def _():
                arrived(rd.at[k, at], rd_r.at[line, k])
                es[k, at, :] += rd[k, at, :]
                send(es.at[k, at], rd.at[k, at], rd_s.at[line], rd_r.at[line, k], down)

    def finish_expr(k):
        at = block(z)
        ge[k] = es[k, at, :]

        @pl.when(z > 0)
        def _():
            arrived(ru.at[k, at], ru_r.at[z, k])
            ge[k] += ru[k, at, :]

        @pl.when(z < last)
        def _():
            arrived(rd.at[k, at], rd_r.at[z, k])
            ge[k] += rd[k, at, :]

        pltpu.make_async_copy(ge.at[k], gexp_ref.at[:, cols(k)], out_s.at[slides]).start()

    added = 0
    for k in range(chunks):
        backward_product(k)
        while 3 * (added + 1) <= 2 * k:
            add_on(added)
            added += 1

    for p in mates:
        send(fs.at[share(p)], fr.at[q], f_s, f_r.at[q], mate(p))
    fr[q] = fs[share(q), :]
    send(fr.at[q], fo.at[q], fo_s, fo_r.at[q], sibling)
    for p in mates:
        arrived(l1.at[p], l1_r.at[p])
    l2[z] = (l1[0] + l1[1]) + (l1[2] + l1[3])
    for o in others:
        send(l2.at[z], l2.at[z], l2_s, l2_r.at[z], (o * PLANE + q, core))
    while added < chunks - 1:
        add_on(added)
        added += 1
    for p in (mates[1], mates[2], mates[0]):
        arrived(fr.at[p], f_r.at[p])
        send(fr.at[p], fo.at[p], fo_s, fo_r.at[p], sibling)
    add_on(chunks - 1)
    for k in range(chunks - 1):
        finish_expr(k)

    arrived(inn.at[1 - core], in_r)
    both = inn[0] + inn[1]
    rowv[1] = jnp.broadcast_to(dmass, (rows, LANES))
    rowv[2] = jnp.broadcast_to(both[:, 0:1] + dmass * mass, (rows, LANES))
    for p in range(PLANE):
        arrived(fo.at[p], fo_r.at[p])

    @pl.loop(0, rows // STEP_ROWS)
    def _(step):
        at = pl.ds(pl.multiple_of(step * STEP_ROWS, STEP_ROWS), STEP_ROWS)
        by_mass, total_inner = rowv[1, at, 0:1], rowv[2, at, 0:1]
        for p in range(PLANE):
            for line in range(lines):
                here, there = pl.ds(line * cb, cb), (line * PLANE + p) * cb
                grad = fr[p, at, here] + fo[p, at, here] + by_mass * weights[:, there : there + cb]
                go[at, pl.ds(there, cb)] = pq[p, at, here] * (grad - total_inner)

    for m in range(slides):
        part = pl.ds(m * slide_rows, slide_rows)
        pltpu.make_async_copy(go.at[part], glog_ref.at[m], out_s.at[slides + 1 + m]).start()

    for o in others:
        arrived(l2.at[o], l2_r.at[o])
    loss = l2[0]
    for line in range(1, lines):
        loss = loss + l2[line]
    loss_ref[...] = loss[0:1, 0:1] - both[0:1, 1:2]
    finish_expr(chunks - 1)

    for m in range(slides):
        part = pl.ds(m * slide_rows, slide_rows)
        pltpu.make_async_copy(pr.at[:, part], pr.at[:, part], out_s.at[m]).wait()
        pltpu.make_async_copy(go.at[part], glog_ref.at[m], out_s.at[slides + 1 + m]).wait()
    pltpu.make_async_copy(ge, ge, out_s.at[slides]).wait()
    for line in range(lines):
        at = block(line)

        @pl.when((line <= z) & (z < last))
        def _():
            sent(bb.at[:, at], ag_us.at[line])

        @pl.when((line >= z) & (z > 0))
        def _():
            sent(bb.at[:, at], ag_ds.at[line])

        @pl.when(line > z)
        def _():
            sent(es.at[:, at], ru_s.at[line])

        @pl.when(line < z)
        def _():
            sent(es.at[:, at], rd_s.at[line])

    three = pl.ds(0, len(mates))
    sent(ab.at[three], a_s)
    sent(cr.at[:, three], c_s)
    sent(s1.at[three], s1_s)
    sent(s2.at[pl.ds(0, last)], s2_s)
    sent(ss.at[0], ss_s)
    sent(ds.at[:, three], d_s)
    sent(inn.at[0], in_s)
    sent(l1.at[three], l1_s)
    sent(l2.at[pl.ds(0, last)], l2_s)
    sent(fr.at[three], f_s)
    sent(fo, fo_s)


def plane_call(logits, expr, spatial, slide_spots, spot_cells, cell_prior, lines, chunks):
    slides, slide_rows, cells = logits.shape
    rows = slides * slide_rows
    cb, genes = expr.shape
    width = genes // chunks
    quarter = lines * cb
    spots = PLANE * rows
    dma = pltpu.SemaphoreType.DMA
    vmem = pltpu.VMEM
    anywhere = pl.BlockSpec(memory_space=pl.ANY)
    in_vmem = pl.BlockSpec(memory_space=pltpu.VMEM)
    scratch = [
        vmem((rows, cells), F32),
        vmem((rows, genes), F32),
        vmem((PLANE, rows, quarter), F32),
        vmem((PLANE, rows, quarter), F32),
        vmem((spots, quarter), BF16),
        vmem((spots, quarter), BF16),
        vmem((quarter, spots), BF16),
        vmem((quarter, spots), BF16),
        vmem((chunks, quarter, width), F32),
        vmem((chunks, quarter, width), BF16),
        vmem((chunks, quarter, width), BF16),
        vmem((chunks, spots, width), F32),
        vmem((chunks, PLANE, rows, width), F32),
        vmem((chunks, rows, width), F32),
        vmem((3, rows, width), F32),
        vmem((PLANE, 8, genes), F32),
        vmem((lines, 8, genes), F32),
        vmem((8, genes), F32),
        vmem((2, rows, LANES), F32),
        vmem((3, rows, LANES), F32),
        vmem((chunks, PLANE, rows, width), F32),
        vmem((chunks, quarter, width), F32),
        vmem((chunks, quarter, width), F32),
        vmem((chunks, quarter, width), F32),
        vmem((spots, quarter), F32),
        vmem((PLANE, rows, quarter), F32),
        vmem((PLANE, rows, quarter), F32),
        vmem((rows, cells), F32),
        vmem((chunks, cb, width), F32),
        vmem((2, rows, LANES), F32),
        vmem((PLANE, 8, LANES), F32),
        vmem((lines, 8, LANES), F32),
        dma((2 * slides,)),
        dma((chunks,)),
        dma((lines, chunks)),
        dma((lines,)),
        dma((lines,)),
        dma,
        dma((PLANE,)),
        dma,
        dma((chunks, PLANE)),
        dma,
        dma((PLANE,)),
        dma,
        dma((lines,)),
        dma,
        dma,
        dma,
        dma((chunks, PLANE)),
        dma((lines,)),
        dma((lines, chunks)),
        dma((lines,)),
        dma((lines, chunks)),
        dma,
        dma((PLANE,)),
        dma,
        dma((PLANE,)),
        dma,
        dma,
        dma,
        dma((PLANE,)),
        dma,
        dma((lines,)),
        dma((2 * slides + 1,)),
    ]
    pred, loss, grad_logits, grad_expr = pl.pallas_call(
        functools.partial(plane_kernel, lines, chunks),
        out_shape=(
            jax.ShapeDtypeStruct((slides, slide_rows, genes), F32),
            jax.ShapeDtypeStruct((1, 1), F32),
            jax.ShapeDtypeStruct((slides, slide_rows, cells), F32),
            jax.ShapeDtypeStruct((cb, genes), F32),
        ),
        in_specs=[
            anywhere,
            anywhere,
            anywhere,
            pl.BlockSpec(memory_space=pltpu.SMEM),
            in_vmem,
            in_vmem,
        ],
        out_specs=(anywhere, in_vmem, anywhere, anywhere),
        scratch_shapes=scratch,
        compiler_params=pltpu.CompilerParams(
            collective_id=0, has_side_effects=True, vmem_limit_bytes=56 * 1024 * 1024
        ),
    )(logits, expr, spatial, slide_spots, spot_cells, cell_prior.reshape(1, cells))
    return pred, loss.reshape(()), grad_logits, grad_expr


def general_plan(logits, expr, spatial, slide_spots, spot_cells, cell_prior):
    place = lax.axis_index("spot")
    side = lax.axis_index("gene")
    rows_all = logits.shape[1]
    cell_rows = expr.shape[0]
    weights = cell_prior.astype(jnp.float32) / fixed_point
    gene_share = (place == 0).astype(jnp.float32)
    row_share = (side == 0).astype(jnp.float32)
    own_weights = lax.dynamic_slice_in_dim(weights, place * cell_rows, cell_rows, 0)
    expr_acc = jnp.zeros((cell_rows, expr.shape[1]), jnp.float32)
    loss_local = jnp.zeros((), jnp.float32)
    pred_list = []
    grad_list = []
    for slide in range(logits.shape[0]):
        logit_rows = logits[slide]
        counted = spot_cells[slide].astype(jnp.float32)
        target = spatial[slide]
        positions = place * rows_all + jnp.arange(rows_all, dtype=jnp.int32)
        valid = (positions < slide_spots[slide]).astype(jnp.float32)
        peak = jnp.max(logit_rows, axis=1, keepdims=True)
        raised = jnp.exp(logit_rows - peak)
        probs = raised / jnp.sum(raised, axis=1, keepdims=True)
        mass = jnp.dot(probs, weights, precision=lax.Precision.HIGHEST)
        blocks = lax.all_to_all(probs, "spot", split_axis=1, concat_axis=0, tiled=True)
        pred = lax.psum_scatter(
            jnp.dot(blocks, expr, precision=lax.Precision.HIGHEST),
            "spot",
            scatter_dimension=0,
            tiled=True,
        )
        gene_dot = jnp.sum(valid[:, None] * pred * target, axis=0)
        gene_pred = jnp.sum(valid[:, None] * pred * pred, axis=0)
        gene_true = jnp.sum(valid[:, None] * target * target, axis=0)
        mass_part = jnp.sum(valid * mass)
        kcell = valid * counted
        cell_part = jnp.sum(kcell)
        spot_dot = jnp.sum(pred * target, axis=1)
        spot_pred = jnp.sum(pred * pred, axis=1)
        spot_true = jnp.sum(target * target, axis=1)
        gene_dot, gene_pred, gene_true, mass_total, cell_total = lax.psum(
            (gene_dot, gene_pred, gene_true, mass_part, cell_part), "spot"
        )
        spot_dot, spot_pred, spot_true = lax.psum((spot_dot, spot_pred, spot_true), "gene")
        gene_inv = lax.rsqrt(gene_pred * gene_true + tiny)
        cos_gene = gene_dot * gene_inv
        spot_inv = lax.rsqrt(spot_pred * spot_true + tiny)
        cos_spot = spot_dot * spot_inv
        share = kcell / cell_total
        scale_count = slide_spots[slide].astype(jnp.float32)
        kl_part = jnp.sum(
            share * (jnp.log(counted) - jnp.log(cell_total) - jnp.log(mass) + jnp.log(mass_total))
        )
        loss_local = loss_local - gene_share * jnp.sum(cos_gene)
        loss_local = loss_local + row_share * (scale_count * kl_part - jnp.sum(valid * cos_spot))
        gene_back = cos_gene * gene_true / (gene_pred * gene_true + tiny)
        spot_back = cos_spot * spot_true / (spot_pred * spot_true + tiny)
        dpred = -valid[:, None] * (
            target * (gene_inv[None, :] + spot_inv[:, None])
            - pred * gene_back[None, :]
            - pred * spot_back[:, None]
        )
        dmass = scale_count * valid * (1.0 / mass_total - share / mass)
        pred_list.append(pred)
        grads_full, mass_full = (
            lax.all_gather(dpred, "spot", axis=0, tiled=True),
            lax.all_gather(dmass, "spot", axis=0, tiled=True),
        )
        dprob_cells = jnp.dot(grads_full, expr.T, precision=lax.Precision.HIGHEST)
        dprob_cells = lax.psum(dprob_cells, "gene")
        expr_acc = expr_acc + lax.dot_general(
            blocks, grads_full, (((0,), (0,)), ((), ())), precision=lax.Precision.HIGHEST
        )
        dprob_cells = dprob_cells + mass_full[:, None] * own_weights[None, :]
        dprob_rows = lax.all_to_all(dprob_cells, "spot", split_axis=0, concat_axis=1, tiled=True)
        inner = jnp.sum(probs * dprob_rows, axis=1, keepdims=True)
        dlogit = probs * (dprob_rows - inner)
        grad_list.append(dlogit)
    loss = lax.psum(loss_local, ("spot", "gene"))
    return (jnp.stack(pred_list), loss, jnp.stack(grad_list), expr_acc)


def solution(mesh):
    places = mesh.shape["spot"]

    def on_device(logits, expr, spatial, slide_spots, spot_cells, cell_prior):
        if places == PLANE * PLANE and mesh.shape["gene"] == 2 and logits.shape[2] * expr.shape[1] <= 1 << 21:
            return plane_call(
                logits, expr, spatial, slide_spots, spot_cells, cell_prior, places // PLANE, CHUNKS
            )
        return general_plan(logits, expr, spatial, slide_spots, spot_cells, cell_prior)

    in_specs = (
        P(None, "spot", None),
        P("spot", "gene"),
        P(None, "spot", "gene"),
        P(),
        P(None, "spot"),
        P(),
    )
    out_specs = (P(None, "spot", "gene"), P(), P(None, "spot", None), P("spot", "gene"))
    return jax.shard_map(
        on_device, mesh=mesh, in_specs=in_specs, out_specs=out_specs, check_vma=False
    )
```

```python
import functools

import jax
import jax.numpy as jnp
from jax import lax
from jax.experimental import pallas as pl
from jax.experimental.pallas import tpu as pltpu
from jax.sharding import PartitionSpec as P

tiny = 1e-06
fixed_point = 16384.0
F32 = jnp.float32
BF16 = jnp.bfloat16
MESH = pl.DeviceIdType.MESH

PLANE = 4
LANES = 128
STEP_ROWS = 16
CHUNKS = 8
LEAD = 4
LAG = 2


def halves(value):
    high = value.astype(BF16)
    return high, (value - high.astype(F32)).astype(BF16)


def product(a_high, a_low, b_high, b_low, contract):
    def one(a, b):
        return lax.dot_general(a, b, (contract, ((), ())), preferred_element_type=F32)

    return one(a_high, b_high) + (one(a_high, b_low) + one(a_low, b_high))


def plane_kernel(lines, chunks, *refs):
    (
        (logits_ref, expr_ref, spatial_ref, count_ref, cells_ref, prior_ref),
        (pred_ref, loss_ref, glog_ref, gexp_ref),
        (lg, tg, pq, ab, af, ahi, alo, thi, tlo, bb, bhi, blo, cs, cr, pr, sacc, s1, s2, gv, ss, rowv, rs),
        (ds, dhi, dlo, es, ru, rd, fs, fr, fo, go, ge, inn, l1, l2),
        (loc, ag_r, ag_us, ag_ds, a_s, a_r, a2_s, a2_r, r_s, r_r, c_s, c_r, s1_s, s1_r, s2_s, s2_r, ss_s, ss_r),
        (d_s, d_r, ru_s, ru_r, rd_s, rd_r, f_s, f_r, fo_s, fo_r, in_s, in_r, l1_s, l1_r, l2_s, l2_r, out_s),
    ) = grouped(refs, (6, 4, 22, 14, 18, 17))
    place = lax.axis_index("spot")
    core = lax.axis_index("gene")
    z = place // PLANE
    q = place % PLANE
    col, row = q % 2, q // 2
    mates = ((1 - row) * 2 + 1 - col, row * 2 + 1 - col, (1 - row) * 2 + col)
    others = tuple((z + step) % lines for step in range(1, lines))
    up, down = (place + PLANE, core), (place - PLANE, core)
    sibling = (place, 1 - core)
    slides, slide_rows = logits_ref.shape[0], logits_ref.shape[1]
    rows = slides * slide_rows
    cb = expr_ref.shape[0]
    genes = expr_ref.shape[1]
    width = genes // chunks
    last = lines - 1
    at_end = (z == 0) | (z == last)
    in_middle = (z > 0) & (z < last)

    def mate(p):
        return (z * PLANE + p, core)

    def send(src, dst, send_sem, recv_sem, device):
        copy = pltpu.make_async_remote_copy(
            src_ref=src, dst_ref=dst, send_sem=send_sem, recv_sem=recv_sem, device_id=device, device_id_type=MESH
        )
        copy.start()

    def arrived(dst, recv_sem):
        pltpu.make_async_copy(dst, dst, recv_sem).wait()

    sent = arrived

    def cols(k):
        return pl.ds(k * width, width)

    def block(index):
        return pl.ds(pl.multiple_of(index * cb, cb), cb)

    def share(index):
        return pl.ds(pl.multiple_of(index * rows, rows), rows)

    def half(index):
        return pl.ds(pl.multiple_of(index * slide_rows, slide_rows), slide_rows)

    for m in range(slides):
        pltpu.make_async_copy(logits_ref.at[m], lg.at[half(m)], loc.at[m]).start()
        pltpu.make_async_copy(spatial_ref.at[m], tg.at[half(m)], loc.at[slides + m]).start()
    pltpu.make_async_copy(expr_ref, bb.at[block(z)], loc.at[2 * slides]).start()

    barrier = pltpu.get_barrier_semaphore()
    for p in mates:
        pl.semaphore_signal(barrier, inc=1, device_id=mate(p), device_id_type=MESH)
    for o in others:
        pl.semaphore_signal(barrier, inc=1, device_id=(o * PLANE + q, core), device_id_type=MESH)
    pl.semaphore_signal(barrier, inc=1, device_id=sibling, device_id_type=MESH)
    pl.semaphore_wait(barrier, len(mates) + len(others) + 1)

    for p in mates:
        for line in range(lines):
            there = pl.ds(pl.multiple_of((line * PLANE + p) * cb, cb), cb)
            send(
                logits_ref.at[core, :, there],
                ab.at[q, half(core), pl.ds(line * cb, cb)],
                a_s,
                a_r.at[q],
                mate(p),
            )

    def send_own(k):
        here = bb.at[block(z), cols(k)]

        @pl.when(z < last)
        def _():
            send(expr_ref.at[:, cols(k)], here, ag_us.at[z], ag_r.at[z, k], up)

        @pl.when(z > 0)
        def _():
            send(expr_ref.at[:, cols(k)], here, ag_ds.at[z], ag_r.at[z, k], down)

    for k in range(min(LEAD, chunks)):
        send_own(k)

    @pl.when(at_end)
    def _():
        for k in range(LEAD, chunks):
            send_own(k)

    def forward(k):
        @pl.when(in_middle)
        def _():
            for distance in range(1, last):
                below, above = z - distance, z + distance

                @pl.when(below >= 0)
                def _():
                    here = bb.at[block(below), cols(k)]
                    arrived(here, ag_r.at[below, k])
                    send(here, here, ag_us.at[below], ag_r.at[below, k], up)

                @pl.when(above <= last)
                def _():
                    here = bb.at[block(above), cols(k)]
                    arrived(here, ag_r.at[above, k])
                    send(here, here, ag_ds.at[above], ag_r.at[above, k], down)

            if k + LEAD < chunks:
                send_own(k + LEAD)

    def gathered(k):
        @pl.when(at_end)
        def _():
            for distance in range(1, lines):
                line = jnp.where(z == 0, distance, last - distance)
                arrived(bb.at[block(line), cols(k)], ag_r.at[line, k])

    weights = prior_ref[...].astype(F32) / fixed_point
    for m in range(slides):
        pltpu.make_async_copy(logits_ref.at[m], lg.at[half(m)], loc.at[m]).wait()

    @pl.loop(0, rows // STEP_ROWS)
    def _(step):
        at = pl.ds(pl.multiple_of(step * STEP_ROWS, STEP_ROWS), STEP_ROWS)
        value = lg[at, :]
        peak = jnp.max(value, axis=1, keepdims=True)
        raised = jnp.exp(value - peak)
        scale = 1.0 / jnp.sum(raised, axis=1, keepdims=True)
        probs = raised * scale
        mass_rows = jnp.sum(probs * weights, axis=1, keepdims=True)
        rowv[0, at, :] = jnp.broadcast_to(mass_rows, (STEP_ROWS, LANES))
        rowv[1, at, :] = jnp.broadcast_to(peak, (STEP_ROWS, LANES))
        rowv[2, at, :] = jnp.broadcast_to(scale, (STEP_ROWS, LANES))
        for p in range(PLANE):
            for line in range(lines):
                at_cells = (line * PLANE + p) * cb
                pq[p, at, pl.ds(line * cb, cb)] = probs[:, at_cells : at_cells + cb]

    wide = lax.broadcasted_iota(jnp.int32, (rows, LANES), 1)
    rs[q] = jnp.where(wide == 0, rowv[1], rowv[2]).T[0:8]
    for p in mates:
        send(rs.at[q], rs.at[q], r_s, r_r.at[q], mate(p))

    for p in (mates[1], mates[2], mates[0]):
        here = ab.at[p, half(core)]
        arrived(here, a_r.at[p])
        send(here, here, a2_s, a2_r.at[p], sibling)
    forward(0)

    rid = lax.broadcasted_iota(jnp.int32, (rows, 1), 0)
    first = rid < slide_rows
    position = place * slide_rows + jnp.where(first, rid, rid - slide_rows)
    count = jnp.where(first, count_ref[0], count_ref[1])
    valid = (position < count).astype(F32)
    scale_count = count.astype(F32)
    square = (slide_rows, slide_rows)
    eye = lax.broadcasted_iota(jnp.int32, square, 0) == lax.broadcasted_iota(jnp.int32, square, 1)
    counted = jnp.concatenate(
        [
            jnp.sum(jnp.where(eye, cells_ref[m : m + 1, :].astype(F32), 0.0), axis=1, keepdims=True)
            for m in range(slides)
        ],
        axis=0,
    )
    mass = rowv[0, :, 0:1]
    kcell = valid * counted

    def by_slide(value):
        return [jnp.sum(value[m * slide_rows : (m + 1) * slide_rows], axis=0, keepdims=True) for m in range(slides)]

    mass_parts = by_slide(valid * mass)
    cell_parts = by_slide(kcell)
    lane = lax.broadcasted_iota(jnp.int32, (1, width), 1)
    scalars = jnp.zeros((1, width), F32)
    for at, value in enumerate(mass_parts + cell_parts):
        scalars = jnp.where(lane == at, value, scalars)
    for m in range(slides):
        pltpu.make_async_copy(spatial_ref.at[m], tg.at[half(m)], loc.at[slides + m]).wait()
    sacc[...] = jnp.zeros_like(sacc)
    pltpu.make_async_copy(expr_ref, bb.at[block(z)], loc.at[2 * slides]).wait()

    af[q] = pq[q]
    ahi[share(q), :], alo[share(q), :] = halves(pq[q])
    for p in (mates[1], mates[2], mates[0]):
        arrived(rs.at[p], r_r.at[p])
        arrived(ab.at[p, half(1 - core)], a2_r.at[p])
        by_row = rs[p].T
        probs = jnp.exp(ab[p] - by_row[:, 0:1]) * by_row[:, 1:2]
        af[p] = probs
        ahi[share(p), :], alo[share(p), :] = halves(probs)

    def forward_product(k):
        gathered(k)
        high, low = halves(bb[:, cols(k)])
        bhi[:, cols(k)], blo[:, cols(k)] = high, low
        cs[:, cols(k)] = product(ahi[...], alo[...], high, low, ((1,), (0,)))
        for p in mates:
            send(cs.at[share(p), cols(k)], cr.at[q, :, cols(k)], c_s, c_r.at[k, q], mate(p))

    def finish_pred(k):
        total = cs[share(q), cols(k)]
        for p in mates:
            arrived(cr.at[p, :, cols(k)], c_r.at[k, p])
            total = total + cr[p, :, cols(k)]
        pr[:, cols(k)] = total
        truth = tg[:, cols(k)]
        for m in range(slides):
            pltpu.make_async_copy(pr.at[half(m), cols(k)], pred_ref.at[m, :, cols(k)], out_s.at[m]).start()
        sacc[0] += total * truth
        sacc[1] += total * total
        sacc[2] += truth * truth
        kept = valid * total
        stats = by_slide(kept * truth) + by_slide(kept * total) + by_slide(valid * truth * truth)
        s1[q, :, cols(k)] = jnp.concatenate(stats + [scalars, jnp.zeros((1, width), F32)], axis=0)

    early = (chunks - LAG) * width
    parts = (pl.ds(0, early), pl.ds(early, genes - early))

    def sum_plane(at):
        for p in mates:
            send(s1.at[q, :, parts[at]], s1.at[q, :, parts[at]], s1_s, s1_r.at[at, q], mate(p))

    def sum_line(at):
        for p in mates:
            arrived(s1.at[p, :, parts[at]], s1_r.at[at, p])
        s2[z, :, parts[at]] = (s1[0, :, parts[at]] + s1[1, :, parts[at]]) + (s1[2, :, parts[at]] + s1[3, :, parts[at]])
        for o in others:
            send(s2.at[z, :, parts[at]], s2.at[z, :, parts[at]], s2_s, s2_r.at[at, z], (o * PLANE + q, core))

    for k in range(chunks):
        if k + 1 < chunks:
            forward(k + 1)
        forward_product(k)
        if k >= LAG:
            finish_pred(k - LAG)
    sum_plane(0)
    for p in range(PLANE):
        high, low = halves(af[p].T)
        thi[:, share(p)], tlo[:, share(p)] = high, low
    finish_pred(chunks - 2)
    sum_line(0)
    finish_pred(chunks - 1)
    sum_plane(1)

    sums = [jnp.sum(sacc[at], axis=1, keepdims=True) for at in range(3)]
    ss[core] = jnp.where(wide == 0, sums[0], jnp.where(wide == 1, sums[1], sums[2]))
    send(ss.at[core], ss.at[core], ss_s, ss_r, sibling)
    sum_line(1)
    arrived(ss.at[1 - core], ss_r)
    spot = ss[0] + ss[1]
    spot_dot, spot_pred, spot_true = spot[:, 0:1], spot[:, 1:2], spot[:, 2:3]
    spot_inv = lax.rsqrt(spot_pred * spot_true + tiny)
    cos_spot = spot_dot * spot_inv
    spot_back = cos_spot * spot_true / (spot_pred * spot_true + tiny)
    for o in others:
        for at in range(2):
            arrived(s2.at[o, :, parts[at]], s2_r.at[at, o])
    total = s2[0]
    for line in range(1, lines):
        total = total + s2[line]
    gene_dot, gene_pred, gene_true = total[0:2], total[2:4], total[4:6]
    gene_inv = lax.rsqrt(gene_pred * gene_true + tiny)
    cos_gene = gene_dot * gene_inv
    gv[0:2, :] = gene_inv
    gv[2:4, :] = cos_gene * gene_true / (gene_pred * gene_true + tiny)

    inner = jnp.zeros((rows, 1), F32)
    for k in range(chunks):
        pieces = []
        for m in range(slides):
            lo, hi = m * slide_rows, (m + 1) * slide_rows
            truth, guess = tg[lo:hi, cols(k)], pr[lo:hi, cols(k)]
            inverse, back = gv[m : m + 1, cols(k)], gv[2 + m : 3 + m, cols(k)]
            pieces.append(
                -valid[lo:hi]
                * (truth * (inverse + spot_inv[lo:hi]) - guess * back - guess * spot_back[lo:hi])
            )
        grad = jnp.concatenate(pieces, axis=0)
        here = ds.at[share(q), cols(k)]
        here[...] = grad
        for p in mates:
            send(here, here, d_s, d_r.at[k, q], mate(p))
        inner = inner + jnp.sum(grad * pr[:, cols(k)], axis=1, keepdims=True)
    gene_sum = jnp.sum(jnp.sum(cos_gene, axis=1, keepdims=True), axis=0, keepdims=True)
    inn[core] = jnp.where(wide == 0, inner, gene_sum)
    send(inn.at[core], inn.at[core], in_s, in_r, sibling)

    mass_total = jnp.where(first, total[6:7, 0:1], total[6:7, 1:2])
    cell_total = jnp.where(first, total[6:7, 2:3], total[6:7, 3:4])
    portion = kcell / cell_total
    kl_rows = portion * (jnp.log(counted) - jnp.log(cell_total) - jnp.log(mass) + jnp.log(mass_total))
    dmass = scale_count * valid * (1.0 / mass_total - portion / mass)
    terms = jnp.sum(scale_count * kl_rows - valid * cos_spot, axis=0, keepdims=True)
    l1[q] = jnp.broadcast_to(terms, (8, LANES))
    for p in mates:
        send(l1.at[q], l1.at[q], l1_s, l1_r.at[q], mate(p))

    def backward_product(k):
        for p in mates:
            arrived(ds.at[share(p), cols(k)], d_r.at[k, p])
        high, low = halves(ds[:, cols(k)])
        dhi[:, cols(k)], dlo[:, cols(k)] = high, low
        es[:, cols(k)] = product(thi[...], tlo[...], high, low, ((1,), (0,)))

        @pl.when(z == 0)
        def _():
            for line in range(last, 0, -1):
                there = ru.at[block(line), cols(k)]
                send(es.at[block(line), cols(k)], there, ru_s.at[line], ru_r.at[line, k], up)

        @pl.when(z == last)
        def _():
            for line in range(last):
                there = rd.at[block(line), cols(k)]
                send(es.at[block(line), cols(k)], there, rd_s.at[line], rd_r.at[line, k], down)

    def add_on(k):
        for line in range(last, 1, -1):
            at = block(line)

            @pl.when((z > 0) & (z < line))
            def _():
                arrived(ru.at[at, cols(k)], ru_r.at[line, k])
                es[at, cols(k)] += ru[at, cols(k)]
                send(es.at[at, cols(k)], ru.at[at, cols(k)], ru_s.at[line], ru_r.at[line, k], up)

        for line in range(last - 1):
            at = block(line)

            @pl.when((z < last) & (z > line))
            def _():
                arrived(rd.at[at, cols(k)], rd_r.at[line, k])
                es[at, cols(k)] += rd[at, cols(k)]
                send(es.at[at, cols(k)], rd.at[at, cols(k)], rd_s.at[line], rd_r.at[line, k], down)

    def finish_expr(k):
        at = block(z)
        ge[:, cols(k)] = es[at, cols(k)]

        @pl.when(z > 0)
        def _():
            arrived(ru.at[at, cols(k)], ru_r.at[z, k])
            ge[:, cols(k)] += ru[at, cols(k)]

        @pl.when(z < last)
        def _():
            arrived(rd.at[at, cols(k)], rd_r.at[z, k])
            ge[:, cols(k)] += rd[at, cols(k)]

        pltpu.make_async_copy(ge.at[:, cols(k)], gexp_ref.at[:, cols(k)], out_s.at[slides]).start()

    def probs_gradient(at):
        return product(dhi[:, at], dlo[:, at], bhi[:, at], blo[:, at], ((1,), (1,)))

    added = 0
    middle = chunks // 2
    for k in range(chunks):
        backward_product(k)
        if k == middle - 1:
            fs[...] = probs_gradient(pl.ds(0, middle * width))
        while 3 * (added + 1) <= 2 * k:
            add_on(added)
            added += 1
    fs[...] += probs_gradient(pl.ds(middle * width, genes - middle * width))

    for p in mates:
        send(fs.at[share(p)], fr.at[q], f_s, f_r.at[q], mate(p))
    fr[q] = fs[share(q), :]
    send(fr.at[q], fo.at[q], fo_s, fo_r.at[q], sibling)
    for p in mates:
        arrived(l1.at[p], l1_r.at[p])
    l2[z] = (l1[0] + l1[1]) + (l1[2] + l1[3])
    for o in others:
        send(l2.at[z], l2.at[z], l2_s, l2_r.at[z], (o * PLANE + q, core))
    while added < chunks - 1:
        add_on(added)
        added += 1
    for p in (mates[1], mates[2], mates[0]):
        arrived(fr.at[p], f_r.at[p])
        send(fr.at[p], fo.at[p], fo_s, fo_r.at[p], sibling)
    add_on(chunks - 1)
    for k in range(chunks - 2):
        finish_expr(k)

    arrived(inn.at[1 - core], in_r)
    both = inn[0] + inn[1]
    rowv[1] = jnp.broadcast_to(dmass, (rows, LANES))
    rowv[2] = jnp.broadcast_to(both[:, 0:1] + dmass * mass, (rows, LANES))
    for p in range(PLANE):
        arrived(fo.at[p], fo_r.at[p])

    @pl.loop(0, rows // STEP_ROWS)
    def _(step):
        at = pl.ds(pl.multiple_of(step * STEP_ROWS, STEP_ROWS), STEP_ROWS)
        by_mass, total_inner = rowv[1, at, 0:1], rowv[2, at, 0:1]
        for p in range(PLANE):
            for line in range(lines):
                here, there = pl.ds(line * cb, cb), (line * PLANE + p) * cb
                grad = fr[p, at, here] + fo[p, at, here] + by_mass * weights[:, there : there + cb]
                go[at, pl.ds(there, cb)] = pq[p, at, here] * (grad - total_inner)

    for m in range(slides):
        pltpu.make_async_copy(go.at[half(m)], glog_ref.at[m], out_s.at[slides + 1 + m]).start()

    for o in others:
        arrived(l2.at[o], l2_r.at[o])
    loss = l2[0]
    for line in range(1, lines):
        loss = loss + l2[line]
    loss_ref[...] = loss[0:1, 0:1] - both[0:1, 1:2]
    finish_expr(chunks - 2)
    finish_expr(chunks - 1)

    for m in range(slides):
        pltpu.make_async_copy(pr.at[half(m)], pred_ref.at[m], out_s.at[m]).wait()
        pltpu.make_async_copy(go.at[half(m)], glog_ref.at[m], out_s.at[slides + 1 + m]).wait()
    pltpu.make_async_copy(ge, gexp_ref, out_s.at[slides]).wait()
    for line in range(lines):
        at = block(line)

        @pl.when((line <= z) & (z < last))
        def _():
            sent(bb.at[at], ag_us.at[line])

        @pl.when((line >= z) & (z > 0))
        def _():
            sent(bb.at[at], ag_ds.at[line])

        @pl.when(line > z)
        def _():
            sent(es.at[at], ru_s.at[line])

        @pl.when(line < z)
        def _():
            sent(es.at[at], rd_s.at[line])

    three = pl.ds(0, len(mates))
    sent(ab.at[three, half(0)], a_s)
    sent(ab.at[three, half(0)], a2_s)
    sent(rs.at[three], r_s)
    sent(cr.at[three], c_s)
    sent(s1.at[three], s1_s)
    sent(s2.at[pl.ds(0, last)], s2_s)
    sent(ss.at[0], ss_s)
    sent(cr.at[three], d_s)
    sent(inn.at[0], in_s)
    sent(l1.at[three], l1_s)
    sent(l2.at[pl.ds(0, last)], l2_s)
    sent(fr.at[three], f_s)
    sent(fo, fo_s)


def grouped(refs, sizes):
    at = 0
    for size in sizes:
        yield refs[at : at + size]
        at += size


def deliver(pred_in, glog_in, gexp_in, pred_ref, glog_ref, gexp_ref, sems):
    pairs = ((glog_in, glog_ref), (pred_in, pred_ref), (gexp_in, gexp_ref))
    copies = [pltpu.make_async_copy(src, dst, sems.at[at]) for at, (src, dst) in enumerate(pairs)]
    for copy in copies:
        copy.start()
    for copy in copies:
        copy.wait()


def plane_call(logits, expr, spatial, slide_spots, spot_cells, cell_prior, lines, chunks):
    slides, slide_rows, cells = logits.shape
    rows = slides * slide_rows
    cb, genes = expr.shape
    quarter = lines * cb
    spots = PLANE * rows
    width = genes // chunks
    dma = pltpu.SemaphoreType.DMA
    vmem = pltpu.VMEM
    anywhere = pl.BlockSpec(memory_space=pl.ANY)
    in_vmem = pl.BlockSpec(memory_space=pltpu.VMEM)
    in_smem = pl.BlockSpec(memory_space=pltpu.SMEM)
    scratch = [
        vmem((rows, cells), F32),
        vmem((rows, genes), F32),
        vmem((PLANE, rows, quarter), F32),
        vmem((PLANE, rows, quarter), F32),
        vmem((PLANE, rows, quarter), F32),
        vmem((spots, quarter), BF16),
        vmem((spots, quarter), BF16),
        vmem((quarter, spots), BF16),
        vmem((quarter, spots), BF16),
        vmem((quarter, genes), F32),
        vmem((quarter, genes), BF16),
        vmem((quarter, genes), BF16),
        vmem((spots, genes), F32),
        vmem((PLANE, rows, genes), F32),
        vmem((rows, genes), F32),
        vmem((3, rows, width), F32),
        vmem((PLANE, 8, genes), F32),
        vmem((lines, 8, genes), F32),
        vmem((8, genes), F32),
        vmem((2, rows, LANES), F32),
        vmem((3, rows, LANES), F32),
        vmem((PLANE, 8, rows), F32),
        vmem((spots, genes), F32),
        vmem((spots, genes), BF16),
        vmem((spots, genes), BF16),
        vmem((quarter, genes), F32),
        vmem((quarter, genes), F32),
        vmem((quarter, genes), F32),
        vmem((spots, quarter), F32),
        vmem((PLANE, rows, quarter), F32),
        vmem((PLANE, rows, quarter), F32),
        vmem((rows, cells), F32),
        vmem((cb, genes), F32),
        vmem((2, rows, LANES), F32),
        vmem((PLANE, 8, LANES), F32),
        vmem((lines, 8, LANES), F32),
        dma((2 * slides + 1,)),
        dma((lines, chunks)),
        dma((lines,)),
        dma((lines,)),
        dma,
        dma((PLANE,)),
        dma,
        dma((PLANE,)),
        dma,
        dma((PLANE,)),
        dma,
        dma((chunks, PLANE)),
        dma,
        dma((2, PLANE)),
        dma,
        dma((2, lines)),
        dma,
        dma,
        dma,
        dma((chunks, PLANE)),
        dma((lines,)),
        dma((lines, chunks)),
        dma((lines,)),
        dma((lines, chunks)),
        dma,
        dma((PLANE,)),
        dma,
        dma((PLANE,)),
        dma,
        dma,
        dma,
        dma((PLANE,)),
        dma,
        dma((lines,)),
        dma((2 * slides + 1,)),
    ]
    pred_shape = jax.ShapeDtypeStruct((slides, slide_rows, genes), F32)
    glog_shape = jax.ShapeDtypeStruct((slides, slide_rows, cells), F32)
    gexp_shape = jax.ShapeDtypeStruct((cb, genes), F32)
    pred, loss, grad_logits, grad_expr = pl.pallas_call(
        functools.partial(plane_kernel, lines, chunks),
        out_shape=(pred_shape, jax.ShapeDtypeStruct((1, 1), F32), glog_shape, gexp_shape),
        in_specs=[anywhere, anywhere, anywhere, in_smem, in_vmem, in_vmem],
        out_specs=(anywhere, in_vmem, anywhere, anywhere),
        scratch_shapes=scratch,
        compiler_params=pltpu.CompilerParams(
            collective_id=0, has_side_effects=True, vmem_limit_bytes=56 * 1024 * 1024
        ),
    )(logits, expr, spatial, slide_spots, spot_cells, cell_prior.reshape(1, cells))
    pred, grad_logits, grad_expr = pl.pallas_call(
        deliver,
        out_shape=(pred_shape, glog_shape, gexp_shape),
        in_specs=[anywhere] * 3,
        out_specs=(anywhere,) * 3,
        scratch_shapes=[dma((3,))],
        compiler_params=pltpu.CompilerParams(vmem_limit_bytes=56 * 1024 * 1024),
    )(pred, grad_logits, grad_expr)
    return pred, loss.reshape(()), grad_logits, grad_expr


def general_plan(logits, expr, spatial, slide_spots, spot_cells, cell_prior):
    place = lax.axis_index("spot")
    side = lax.axis_index("gene")
    rows_all = logits.shape[1]
    cell_rows = expr.shape[0]
    weights = cell_prior.astype(jnp.float32) / fixed_point
    gene_share = (place == 0).astype(jnp.float32)
    row_share = (side == 0).astype(jnp.float32)
    own_weights = lax.dynamic_slice_in_dim(weights, place * cell_rows, cell_rows, 0)
    expr_acc = jnp.zeros((cell_rows, expr.shape[1]), jnp.float32)
    loss_local = jnp.zeros((), jnp.float32)
    pred_list = []
    grad_list = []
    for slide in range(logits.shape[0]):
        logit_rows = logits[slide]
        counted = spot_cells[slide].astype(jnp.float32)
        target = spatial[slide]
        positions = place * rows_all + jnp.arange(rows_all, dtype=jnp.int32)
        valid = (positions < slide_spots[slide]).astype(jnp.float32)
        peak = jnp.max(logit_rows, axis=1, keepdims=True)
        raised = jnp.exp(logit_rows - peak)
        probs = raised / jnp.sum(raised, axis=1, keepdims=True)
        mass = jnp.dot(probs, weights, precision=lax.Precision.HIGHEST)
        blocks = lax.all_to_all(probs, "spot", split_axis=1, concat_axis=0, tiled=True)
        pred = lax.psum_scatter(
            jnp.dot(blocks, expr, precision=lax.Precision.HIGHEST),
            "spot",
            scatter_dimension=0,
            tiled=True,
        )
        gene_dot = jnp.sum(valid[:, None] * pred * target, axis=0)
        gene_pred = jnp.sum(valid[:, None] * pred * pred, axis=0)
        gene_true = jnp.sum(valid[:, None] * target * target, axis=0)
        mass_part = jnp.sum(valid * mass)
        kcell = valid * counted
        cell_part = jnp.sum(kcell)
        spot_dot = jnp.sum(pred * target, axis=1)
        spot_pred = jnp.sum(pred * pred, axis=1)
        spot_true = jnp.sum(target * target, axis=1)
        gene_dot, gene_pred, gene_true, mass_total, cell_total = lax.psum(
            (gene_dot, gene_pred, gene_true, mass_part, cell_part), "spot"
        )
        spot_dot, spot_pred, spot_true = lax.psum((spot_dot, spot_pred, spot_true), "gene")
        gene_inv = lax.rsqrt(gene_pred * gene_true + tiny)
        cos_gene = gene_dot * gene_inv
        spot_inv = lax.rsqrt(spot_pred * spot_true + tiny)
        cos_spot = spot_dot * spot_inv
        share = kcell / cell_total
        scale_count = slide_spots[slide].astype(jnp.float32)
        kl_part = jnp.sum(
            share * (jnp.log(counted) - jnp.log(cell_total) - jnp.log(mass) + jnp.log(mass_total))
        )
        loss_local = loss_local - gene_share * jnp.sum(cos_gene)
        loss_local = loss_local + row_share * (scale_count * kl_part - jnp.sum(valid * cos_spot))
        gene_back = cos_gene * gene_true / (gene_pred * gene_true + tiny)
        spot_back = cos_spot * spot_true / (spot_pred * spot_true + tiny)
        dpred = -valid[:, None] * (
            target * (gene_inv[None, :] + spot_inv[:, None])
            - pred * gene_back[None, :]
            - pred * spot_back[:, None]
        )
        dmass = scale_count * valid * (1.0 / mass_total - share / mass)
        pred_list.append(pred)
        grads_full, mass_full = (
            lax.all_gather(dpred, "spot", axis=0, tiled=True),
            lax.all_gather(dmass, "spot", axis=0, tiled=True),
        )
        dprob_cells = jnp.dot(grads_full, expr.T, precision=lax.Precision.HIGHEST)
        dprob_cells = lax.psum(dprob_cells, "gene")
        expr_acc = expr_acc + lax.dot_general(
            blocks, grads_full, (((0,), (0,)), ((), ())), precision=lax.Precision.HIGHEST
        )
        dprob_cells = dprob_cells + mass_full[:, None] * own_weights[None, :]
        dprob_rows = lax.all_to_all(dprob_cells, "spot", split_axis=0, concat_axis=1, tiled=True)
        inner = jnp.sum(probs * dprob_rows, axis=1, keepdims=True)
        dlogit = probs * (dprob_rows - inner)
        grad_list.append(dlogit)
    loss = lax.psum(loss_local, ("spot", "gene"))
    return (jnp.stack(pred_list), loss, jnp.stack(grad_list), expr_acc)


def solution(mesh):
    places = mesh.shape["spot"]

    def on_device(logits, expr, spatial, slide_spots, spot_cells, cell_prior):
        if places == PLANE * PLANE and mesh.shape["gene"] == 2 and logits.shape[2] * expr.shape[1] <= 1 << 21:
            return plane_call(
                logits, expr, spatial, slide_spots, spot_cells, cell_prior, places // PLANE, CHUNKS
            )
        return general_plan(logits, expr, spatial, slide_spots, spot_cells, cell_prior)

    in_specs = (
        P(None, "spot", None),
        P("spot", "gene"),
        P(None, "spot", "gene"),
        P(),
        P(None, "spot"),
        P(),
    )
    out_specs = (P(None, "spot", "gene"), P(), P(None, "spot", None), P("spot", "gene"))
    return jax.shard_map(
        on_device, mesh=mesh, in_specs=in_specs, out_specs=out_specs, check_vma=False
    )
```

```python
import functools

import jax
import jax.numpy as jnp
from jax import lax
from jax.experimental import pallas as pl
from jax.experimental.pallas import tpu as pltpu
from jax.sharding import PartitionSpec as P

tiny = 1e-06
fixed_point = 16384.0
F32 = jnp.float32
BF16 = jnp.bfloat16
MESH = pl.DeviceIdType.MESH

PLANE = 4
LANES = 128
STEP_ROWS = 16
CHUNKS = 8
LEAD = 4
LAG = 2


def halves(value):
    high = value.astype(BF16)
    return high, (value - high.astype(F32)).astype(BF16)


def product(a_high, a_low, b_high, b_low, contract):
    def one(a, b):
        return lax.dot_general(a, b, (contract, ((), ())), preferred_element_type=F32)

    return one(a_high, b_high) + (one(a_high, b_low) + one(a_low, b_high))


def plane_kernel(lines, chunks, *refs):
    (
        (logits_ref, expr_ref, spatial_ref, count_ref, cells_ref, prior_ref),
        (pred_ref, loss_ref, glog_ref, gexp_ref),
        (lg, lq, tg, ex, pq, ab, af, ahi, alo, thi, tlo, bb, bhi, blo, cs, cr, pr, sacc, s1, s2, gv, ss, rowv, rs),
        (ds, dhi, dlo, es, ru, rd, fs, fr, fo, go, ge, inn, l1, l2),
        (loc, ag_r, ag_us, ag_ds, a_s, a_r, a2_s, a2_r, r_s, r_r, c_s, c_r, s1_s, s1_r, s2_s, s2_r, ss_s, ss_r),
        (d_s, d_r, ru_s, ru_r, rd_s, rd_r, f_s, f_r, fo_s, fo_r, in_s, in_r, l1_s, l1_r, l2_s, l2_r, out_s),
    ) = grouped(refs, (6, 4, 24, 14, 18, 17))
    place = lax.axis_index("spot")
    core = lax.axis_index("gene")
    z = place // PLANE
    q = place % PLANE
    col, row = q % 2, q // 2
    mates = ((1 - row) * 2 + 1 - col, row * 2 + 1 - col, (1 - row) * 2 + col)
    others = tuple((z + step) % lines for step in range(1, lines))
    up, down = (place + PLANE, core), (place - PLANE, core)
    sibling = (place, 1 - core)
    slides, slide_rows = logits_ref.shape[0], logits_ref.shape[1]
    rows = slides * slide_rows
    cb = expr_ref.shape[0]
    genes = expr_ref.shape[1]
    width = genes // chunks
    last = lines - 1
    at_end = (z == 0) | (z == last)
    in_middle = (z > 0) & (z < last)

    def mate(p):
        return (z * PLANE + p, core)

    def send(src, dst, send_sem, recv_sem, device):
        copy = pltpu.make_async_remote_copy(
            src_ref=src, dst_ref=dst, send_sem=send_sem, recv_sem=recv_sem, device_id=device, device_id_type=MESH
        )
        copy.start()

    def arrived(dst, recv_sem):
        pltpu.make_async_copy(dst, dst, recv_sem).wait()

    sent = arrived

    def cols(k):
        return pl.ds(k * width, width)

    def block(index):
        return pl.ds(pl.multiple_of(index * cb, cb), cb)

    def share(index):
        return pl.ds(pl.multiple_of(index * rows, rows), rows)

    def half(index):
        return pl.ds(pl.multiple_of(index * slide_rows, slide_rows), slide_rows)

    for m in range(slides):
        pltpu.make_async_copy(logits_ref.at[m], lg.at[half(m)], loc.at[m]).start()
        pltpu.make_async_copy(spatial_ref.at[m], tg.at[half(m)], loc.at[slides + m]).start()
    pltpu.make_async_copy(expr_ref, ex, loc.at[2 * slides]).start()

    barrier = pltpu.get_barrier_semaphore()
    for p in mates:
        pl.semaphore_signal(barrier, inc=1, device_id=mate(p), device_id_type=MESH)
    for o in others:
        pl.semaphore_signal(barrier, inc=1, device_id=(o * PLANE + q, core), device_id_type=MESH)
    pl.semaphore_signal(barrier, inc=1, device_id=sibling, device_id_type=MESH)
    pl.semaphore_wait(barrier, len(mates) + len(others) + 1)

    for m in range(slides):
        pltpu.make_async_copy(logits_ref.at[m], lg.at[half(m)], loc.at[m]).wait()
    for p in range(PLANE):
        for line in range(lines):
            lq[p, :, pl.ds(line * cb, cb)] = lg[half(core), pl.ds((line * PLANE + p) * cb, cb)]
    for p in mates:
        send(lq.at[p], ab.at[q, half(core)], a_s, a_r.at[q], mate(p))

    pltpu.make_async_copy(expr_ref, ex, loc.at[2 * slides]).wait()
    for k in range(chunks):
        bb[k, block(z), :] = ex[:, cols(k)]

    def send_own(k):
        here = bb.at[k, block(z)]

        @pl.when(z < last)
        def _():
            send(here, here, ag_us.at[z], ag_r.at[z, k], up)

        @pl.when(z > 0)
        def _():
            send(here, here, ag_ds.at[z], ag_r.at[z, k], down)

    for k in range(min(LEAD, chunks)):
        send_own(k)

    @pl.when(at_end)
    def _():
        for k in range(LEAD, chunks):
            send_own(k)

    def forward(k):
        @pl.when(in_middle)
        def _():
            for distance in range(1, last):
                below, above = z - distance, z + distance

                @pl.when(below >= 0)
                def _():
                    here = bb.at[k, block(below)]
                    arrived(here, ag_r.at[below, k])
                    send(here, here, ag_us.at[below], ag_r.at[below, k], up)

                @pl.when(above <= last)
                def _():
                    here = bb.at[k, block(above)]
                    arrived(here, ag_r.at[above, k])
                    send(here, here, ag_ds.at[above], ag_r.at[above, k], down)

            if k + LEAD < chunks:
                send_own(k + LEAD)

    def gathered(k):
        @pl.when(at_end)
        def _():
            for distance in range(1, lines):
                line = jnp.where(z == 0, distance, last - distance)
                arrived(bb.at[k, block(line)], ag_r.at[line, k])

    weights = prior_ref[...].astype(F32) / fixed_point

    @pl.loop(0, rows // STEP_ROWS)
    def _(step):
        at = pl.ds(pl.multiple_of(step * STEP_ROWS, STEP_ROWS), STEP_ROWS)
        value = lg[at, :]
        peak = jnp.max(value, axis=1, keepdims=True)
        raised = jnp.exp(value - peak)
        scale = 1.0 / jnp.sum(raised, axis=1, keepdims=True)
        probs = raised * scale
        mass_rows = jnp.sum(probs * weights, axis=1, keepdims=True)
        rowv[0, at, :] = jnp.broadcast_to(mass_rows, (STEP_ROWS, LANES))
        rowv[1, at, :] = jnp.broadcast_to(peak, (STEP_ROWS, LANES))
        rowv[2, at, :] = jnp.broadcast_to(scale, (STEP_ROWS, LANES))
        for p in range(PLANE):
            for line in range(lines):
                at_cells = (line * PLANE + p) * cb
                pq[p, at, pl.ds(line * cb, cb)] = probs[:, at_cells : at_cells + cb]

    wide = lax.broadcasted_iota(jnp.int32, (rows, LANES), 1)
    rs[q] = jnp.where(wide == 0, rowv[1], rowv[2]).T[0:8]
    for p in mates:
        send(rs.at[q], rs.at[q], r_s, r_r.at[q], mate(p))

    for p in (mates[1], mates[2], mates[0]):
        here = ab.at[p, half(core)]
        arrived(here, a_r.at[p])
        send(here, here, a2_s, a2_r.at[p], sibling)
    forward(0)

    rid = lax.broadcasted_iota(jnp.int32, (rows, 1), 0)
    first = rid < slide_rows
    position = place * slide_rows + jnp.where(first, rid, rid - slide_rows)
    count = jnp.where(first, count_ref[0], count_ref[1])
    valid = (position < count).astype(F32)
    scale_count = count.astype(F32)
    square = (slide_rows, slide_rows)
    eye = lax.broadcasted_iota(jnp.int32, square, 0) == lax.broadcasted_iota(jnp.int32, square, 1)
    counted = jnp.concatenate(
        [
            jnp.sum(jnp.where(eye, cells_ref[m : m + 1, :].astype(F32), 0.0), axis=1, keepdims=True)
            for m in range(slides)
        ],
        axis=0,
    )
    mass = rowv[0, :, 0:1]
    kcell = valid * counted

    def by_slide(value):
        return [jnp.sum(value[m * slide_rows : (m + 1) * slide_rows], axis=0, keepdims=True) for m in range(slides)]

    mass_parts = by_slide(valid * mass)
    cell_parts = by_slide(kcell)
    lane = lax.broadcasted_iota(jnp.int32, (1, width), 1)
    scalars = jnp.zeros((1, width), F32)
    for at, value in enumerate(mass_parts + cell_parts):
        scalars = jnp.where(lane == at, value, scalars)
    for m in range(slides):
        pltpu.make_async_copy(spatial_ref.at[m], tg.at[half(m)], loc.at[slides + m]).wait()
    sacc[...] = jnp.zeros_like(sacc)

    af[q] = pq[q]
    ahi[share(q), :], alo[share(q), :] = halves(pq[q])
    for p in (mates[1], mates[2], mates[0]):
        arrived(rs.at[p], r_r.at[p])
        arrived(ab.at[p, half(1 - core)], a2_r.at[p])
        by_row = rs[p].T
        probs = jnp.exp(ab[p] - by_row[:, 0:1]) * by_row[:, 1:2]
        af[p] = probs
        ahi[share(p), :], alo[share(p), :] = halves(probs)

    def forward_product(k):
        gathered(k)
        high, low = halves(bb[k])
        bhi[:, cols(k)], blo[:, cols(k)] = high, low
        cs[k] = product(ahi[...], alo[...], high, low, ((1,), (0,)))
        for p in mates:
            send(cs.at[k, share(p)], cr.at[k, q], c_s, c_r.at[k, q], mate(p))

    def finish_pred(k):
        total = cs[k, share(q), :]
        for p in mates:
            arrived(cr.at[k, p], c_r.at[k, p])
            total = total + cr[k, p]
        pr[:, cols(k)] = total
        truth = tg[:, cols(k)]
        sacc[0] += total * truth
        sacc[1] += total * total
        sacc[2] += truth * truth
        kept = valid * total
        stats = by_slide(kept * truth) + by_slide(kept * total) + by_slide(valid * truth * truth)
        s1[q, :, cols(k)] = jnp.concatenate(stats + [scalars, jnp.zeros((1, width), F32)], axis=0)

    early = (chunks - LAG) * width
    parts = (pl.ds(0, early), pl.ds(early, genes - early))

    def sum_plane(at):
        for p in mates:
            send(s1.at[q, :, parts[at]], s1.at[q, :, parts[at]], s1_s, s1_r.at[at, q], mate(p))

    def sum_line(at):
        for p in mates:
            arrived(s1.at[p, :, parts[at]], s1_r.at[at, p])
        s2[z, :, parts[at]] = (s1[0, :, parts[at]] + s1[1, :, parts[at]]) + (s1[2, :, parts[at]] + s1[3, :, parts[at]])
        for o in others:
            send(s2.at[z, :, parts[at]], s2.at[z, :, parts[at]], s2_s, s2_r.at[at, z], (o * PLANE + q, core))

    for k in range(chunks):
        if k + 1 < chunks:
            forward(k + 1)
        forward_product(k)
        if k >= LAG:
            finish_pred(k - LAG)
    sum_plane(0)
    for p in range(PLANE):
        high, low = halves(af[p].T)
        thi[:, share(p)], tlo[:, share(p)] = high, low
    finish_pred(chunks - 2)
    sum_line(0)
    finish_pred(chunks - 1)
    sum_plane(1)
    for m in range(slides):
        pltpu.make_async_copy(pr.at[half(m)], pred_ref.at[m], out_s.at[m]).start()

    sums = [jnp.sum(sacc[at], axis=1, keepdims=True) for at in range(3)]
    ss[core] = jnp.where(wide == 0, sums[0], jnp.where(wide == 1, sums[1], sums[2]))
    send(ss.at[core], ss.at[core], ss_s, ss_r, sibling)
    sum_line(1)
    arrived(ss.at[1 - core], ss_r)
    spot = ss[0] + ss[1]
    spot_dot, spot_pred, spot_true = spot[:, 0:1], spot[:, 1:2], spot[:, 2:3]
    spot_inv = lax.rsqrt(spot_pred * spot_true + tiny)
    cos_spot = spot_dot * spot_inv
    spot_back = cos_spot * spot_true / (spot_pred * spot_true + tiny)
    for o in others:
        for at in range(2):
            arrived(s2.at[o, :, parts[at]], s2_r.at[at, o])
    total = s2[0]
    for line in range(1, lines):
        total = total + s2[line]
    gene_dot, gene_pred, gene_true = total[0:2], total[2:4], total[4:6]
    gene_inv = lax.rsqrt(gene_pred * gene_true + tiny)
    cos_gene = gene_dot * gene_inv
    gv[0:2, :] = gene_inv
    gv[2:4, :] = cos_gene * gene_true / (gene_pred * gene_true + tiny)

    inner = jnp.zeros((rows, 1), F32)
    for k in range(chunks):
        pieces = []
        for m in range(slides):
            lo, hi = m * slide_rows, (m + 1) * slide_rows
            truth, guess = tg[lo:hi, cols(k)], pr[lo:hi, cols(k)]
            inverse, back = gv[m : m + 1, cols(k)], gv[2 + m : 3 + m, cols(k)]
            pieces.append(
                -valid[lo:hi]
                * (truth * (inverse + spot_inv[lo:hi]) - guess * back - guess * spot_back[lo:hi])
            )
        grad = jnp.concatenate(pieces, axis=0)
        here = ds.at[k, share(q)]
        here[...] = grad
        for p in mates:
            send(here, here, d_s, d_r.at[k, q], mate(p))
        inner = inner + jnp.sum(grad * pr[:, cols(k)], axis=1, keepdims=True)
    gene_sum = jnp.sum(jnp.sum(cos_gene, axis=1, keepdims=True), axis=0, keepdims=True)
    inn[core] = jnp.where(wide == 0, inner, gene_sum)
    send(inn.at[core], inn.at[core], in_s, in_r, sibling)

    mass_total = jnp.where(first, total[6:7, 0:1], total[6:7, 1:2])
    cell_total = jnp.where(first, total[6:7, 2:3], total[6:7, 3:4])
    portion = kcell / cell_total
    kl_rows = portion * (jnp.log(counted) - jnp.log(cell_total) - jnp.log(mass) + jnp.log(mass_total))
    dmass = scale_count * valid * (1.0 / mass_total - portion / mass)
    terms = jnp.sum(scale_count * kl_rows - valid * cos_spot, axis=0, keepdims=True)
    l1[q] = jnp.broadcast_to(terms, (8, LANES))
    for p in mates:
        send(l1.at[q], l1.at[q], l1_s, l1_r.at[q], mate(p))

    def backward_product(k):
        for p in mates:
            arrived(ds.at[k, share(p)], d_r.at[k, p])
        high, low = halves(ds[k])
        dhi[:, cols(k)], dlo[:, cols(k)] = high, low
        es[k] = product(thi[...], tlo[...], high, low, ((1,), (0,)))

        @pl.when(z == 0)
        def _():
            for line in range(last, 0, -1):
                there = ru.at[k, block(line)]
                send(es.at[k, block(line)], there, ru_s.at[line], ru_r.at[line, k], up)

        @pl.when(z == last)
        def _():
            for line in range(last):
                there = rd.at[k, block(line)]
                send(es.at[k, block(line)], there, rd_s.at[line], rd_r.at[line, k], down)

    def add_on(k):
        for line in range(last, 1, -1):
            at = block(line)

            @pl.when((z > 0) & (z < line))
            def _():
                arrived(ru.at[k, at], ru_r.at[line, k])
                es[k, at, :] += ru[k, at, :]
                send(es.at[k, at], ru.at[k, at], ru_s.at[line], ru_r.at[line, k], up)

        for line in range(last - 1):
            at = block(line)

            @pl.when((z < last) & (z > line))
            def _():
                arrived(rd.at[k, at], rd_r.at[line, k])
                es[k, at, :] += rd[k, at, :]
                send(es.at[k, at], rd.at[k, at], rd_s.at[line], rd_r.at[line, k], down)

    def finish_expr(k):
        at = block(z)
        ge[:, cols(k)] = es[k, at, :]

        @pl.when(z > 0)
        def _():
            arrived(ru.at[k, at], ru_r.at[z, k])
            ge[:, cols(k)] += ru[k, at, :]

        @pl.when(z < last)
        def _():
            arrived(rd.at[k, at], rd_r.at[z, k])
            ge[:, cols(k)] += rd[k, at, :]

    def probs_gradient(at):
        return product(dhi[:, at], dlo[:, at], bhi[:, at], blo[:, at], ((1,), (1,)))

    added = 0
    middle = chunks // 2
    for k in range(chunks):
        backward_product(k)
        if k == middle - 1:
            fs[...] = probs_gradient(pl.ds(0, middle * width))
        while 3 * (added + 1) <= 2 * k:
            add_on(added)
            added += 1
    fs[...] += probs_gradient(pl.ds(middle * width, genes - middle * width))

    for p in mates:
        send(fs.at[share(p)], fr.at[q], f_s, f_r.at[q], mate(p))
    fr[q] = fs[share(q), :]
    send(fr.at[q], fo.at[q], fo_s, fo_r.at[q], sibling)
    for p in mates:
        arrived(l1.at[p], l1_r.at[p])
    l2[z] = (l1[0] + l1[1]) + (l1[2] + l1[3])
    for o in others:
        send(l2.at[z], l2.at[z], l2_s, l2_r.at[z], (o * PLANE + q, core))
    while added < chunks - 1:
        add_on(added)
        added += 1
    for p in (mates[1], mates[2], mates[0]):
        arrived(fr.at[p], f_r.at[p])
        send(fr.at[p], fo.at[p], fo_s, fo_r.at[p], sibling)
    add_on(chunks - 1)
    for k in range(chunks - 2):
        finish_expr(k)

    arrived(inn.at[1 - core], in_r)
    both = inn[0] + inn[1]
    rowv[1] = jnp.broadcast_to(dmass, (rows, LANES))
    rowv[2] = jnp.broadcast_to(both[:, 0:1] + dmass * mass, (rows, LANES))
    for p in range(PLANE):
        arrived(fo.at[p], fo_r.at[p])

    @pl.loop(0, rows // STEP_ROWS)
    def _(step):
        at = pl.ds(pl.multiple_of(step * STEP_ROWS, STEP_ROWS), STEP_ROWS)
        by_mass, total_inner = rowv[1, at, 0:1], rowv[2, at, 0:1]
        for p in range(PLANE):
            for line in range(lines):
                here, there = pl.ds(line * cb, cb), (line * PLANE + p) * cb
                grad = fr[p, at, here] + fo[p, at, here] + by_mass * weights[:, there : there + cb]
                go[at, pl.ds(there, cb)] = pq[p, at, here] * (grad - total_inner)

    for m in range(slides):
        pltpu.make_async_copy(go.at[half(m)], glog_ref.at[m], out_s.at[slides + 1 + m]).start()

    for o in others:
        arrived(l2.at[o], l2_r.at[o])
    loss = l2[0]
    for line in range(1, lines):
        loss = loss + l2[line]
    loss_ref[...] = loss[0:1, 0:1] - both[0:1, 1:2]
    finish_expr(chunks - 2)
    finish_expr(chunks - 1)
    pltpu.make_async_copy(ge, gexp_ref, out_s.at[slides]).start()

    for m in range(slides):
        pltpu.make_async_copy(pr.at[half(m)], pred_ref.at[m], out_s.at[m]).wait()
        pltpu.make_async_copy(go.at[half(m)], glog_ref.at[m], out_s.at[slides + 1 + m]).wait()
    pltpu.make_async_copy(ge, gexp_ref, out_s.at[slides]).wait()
    for line in range(lines):
        at = block(line)

        @pl.when((line <= z) & (z < last))
        def _():
            sent(bb.at[:, at], ag_us.at[line])

        @pl.when((line >= z) & (z > 0))
        def _():
            sent(bb.at[:, at], ag_ds.at[line])

        @pl.when(line > z)
        def _():
            sent(es.at[:, at], ru_s.at[line])

        @pl.when(line < z)
        def _():
            sent(es.at[:, at], rd_s.at[line])

    three = pl.ds(0, len(mates))
    sent(ab.at[three, half(0)], a_s)
    sent(ab.at[three, half(0)], a2_s)
    sent(rs.at[three], r_s)
    sent(cr.at[:, three], c_s)
    sent(s1.at[three], s1_s)
    sent(s2.at[pl.ds(0, last)], s2_s)
    sent(ss.at[0], ss_s)
    sent(cr.at[:, three], d_s)
    sent(inn.at[0], in_s)
    sent(l1.at[three], l1_s)
    sent(l2.at[pl.ds(0, last)], l2_s)
    sent(fr.at[three], f_s)
    sent(fo, fo_s)


def grouped(refs, sizes):
    at = 0
    for size in sizes:
        yield refs[at : at + size]
        at += size


def deliver(pred_in, glog_in, gexp_in, pred_ref, glog_ref, gexp_ref, pred_mid, glog_mid, gexp_mid, sems):
    triples = ((glog_in, glog_mid, glog_ref), (pred_in, pred_mid, pred_ref), (gexp_in, gexp_mid, gexp_ref))
    loads = [pltpu.make_async_copy(src, mid, sems.at[0, at]) for at, (src, mid, _) in enumerate(triples)]
    stores = [pltpu.make_async_copy(mid, dst, sems.at[1, at]) for at, (_, mid, dst) in enumerate(triples)]
    for load in loads:
        load.start()
    for load, store in zip(loads, stores):
        load.wait()
        store.start()
    for store in stores:
        store.wait()


def plane_call(logits, expr, spatial, slide_spots, spot_cells, cell_prior, lines, chunks):
    slides, slide_rows, cells = logits.shape
    rows = slides * slide_rows
    cb, genes = expr.shape
    quarter = lines * cb
    spots = PLANE * rows
    width = genes // chunks
    dma = pltpu.SemaphoreType.DMA
    vmem = pltpu.VMEM
    anywhere = pl.BlockSpec(memory_space=pl.ANY)
    in_vmem = pl.BlockSpec(memory_space=pltpu.VMEM)
    in_smem = pl.BlockSpec(memory_space=pltpu.SMEM)
    scratch = [
        vmem((rows, cells), F32),
        vmem((PLANE, slide_rows, quarter), F32),
        vmem((rows, genes), F32),
        vmem((cb, genes), F32),
        vmem((PLANE, rows, quarter), F32),
        vmem((PLANE, rows, quarter), F32),
        vmem((PLANE, rows, quarter), F32),
        vmem((spots, quarter), BF16),
        vmem((spots, quarter), BF16),
        vmem((quarter, spots), BF16),
        vmem((quarter, spots), BF16),
        vmem((chunks, quarter, width), F32),
        vmem((quarter, genes), BF16),
        vmem((quarter, genes), BF16),
        vmem((chunks, spots, width), F32),
        vmem((chunks, PLANE, rows, width), F32),
        vmem((rows, genes), F32),
        vmem((3, rows, width), F32),
        vmem((PLANE, 8, genes), F32),
        vmem((lines, 8, genes), F32),
        vmem((8, genes), F32),
        vmem((2, rows, LANES), F32),
        vmem((3, rows, LANES), F32),
        vmem((PLANE, 8, rows), F32),
        vmem((chunks, spots, width), F32),
        vmem((spots, genes), BF16),
        vmem((spots, genes), BF16),
        vmem((chunks, quarter, width), F32),
        vmem((chunks, quarter, width), F32),
        vmem((chunks, quarter, width), F32),
        vmem((spots, quarter), F32),
        vmem((PLANE, rows, quarter), F32),
        vmem((PLANE, rows, quarter), F32),
        vmem((rows, cells), F32),
        vmem((cb, genes), F32),
        vmem((2, rows, LANES), F32),
        vmem((PLANE, 8, LANES), F32),
        vmem((lines, 8, LANES), F32),
        dma((2 * slides + 1,)),
        dma((lines, chunks)),
        dma((lines,)),
        dma((lines,)),
        dma,
        dma((PLANE,)),
        dma,
        dma((PLANE,)),
        dma,
        dma((PLANE,)),
        dma,
        dma((chunks, PLANE)),
        dma,
        dma((2, PLANE)),
        dma,
        dma((2, lines)),
        dma,
        dma,
        dma,
        dma((chunks, PLANE)),
        dma((lines,)),
        dma((lines, chunks)),
        dma((lines,)),
        dma((lines, chunks)),
        dma,
        dma((PLANE,)),
        dma,
        dma((PLANE,)),
        dma,
        dma,
        dma,
        dma((PLANE,)),
        dma,
        dma((lines,)),
        dma((2 * slides + 1,)),
    ]
    pred_shape = jax.ShapeDtypeStruct((slides, slide_rows, genes), F32)
    glog_shape = jax.ShapeDtypeStruct((slides, slide_rows, cells), F32)
    gexp_shape = jax.ShapeDtypeStruct((cb, genes), F32)
    pred, loss, grad_logits, grad_expr = pl.pallas_call(
        functools.partial(plane_kernel, lines, chunks),
        out_shape=(pred_shape, jax.ShapeDtypeStruct((1, 1), F32), glog_shape, gexp_shape),
        in_specs=[anywhere, anywhere, anywhere, in_smem, in_vmem, in_vmem],
        out_specs=(anywhere, in_vmem, anywhere, anywhere),
        scratch_shapes=scratch,
        compiler_params=pltpu.CompilerParams(
            collective_id=0, has_side_effects=True, vmem_limit_bytes=56 * 1024 * 1024
        ),
    )(logits, expr, spatial, slide_spots, spot_cells, cell_prior.reshape(1, cells))
    pred, grad_logits, grad_expr = pl.pallas_call(
        deliver,
        out_shape=(pred_shape, glog_shape, gexp_shape),
        in_specs=[anywhere] * 3,
        out_specs=(anywhere,) * 3,
        scratch_shapes=[vmem(shape.shape, F32) for shape in (pred_shape, glog_shape, gexp_shape)] + [dma((2, 3))],
        compiler_params=pltpu.CompilerParams(vmem_limit_bytes=56 * 1024 * 1024),
    )(pred, grad_logits, grad_expr)
    return pred, loss.reshape(()), grad_logits, grad_expr


def general_plan(logits, expr, spatial, slide_spots, spot_cells, cell_prior):
    place = lax.axis_index("spot")
    side = lax.axis_index("gene")
    rows_all = logits.shape[1]
    cell_rows = expr.shape[0]
    weights = cell_prior.astype(jnp.float32) / fixed_point
    gene_share = (place == 0).astype(jnp.float32)
    row_share = (side == 0).astype(jnp.float32)
    own_weights = lax.dynamic_slice_in_dim(weights, place * cell_rows, cell_rows, 0)
    expr_acc = jnp.zeros((cell_rows, expr.shape[1]), jnp.float32)
    loss_local = jnp.zeros((), jnp.float32)
    pred_list = []
    grad_list = []
    for slide in range(logits.shape[0]):
        logit_rows = logits[slide]
        counted = spot_cells[slide].astype(jnp.float32)
        target = spatial[slide]
        positions = place * rows_all + jnp.arange(rows_all, dtype=jnp.int32)
        valid = (positions < slide_spots[slide]).astype(jnp.float32)
        peak = jnp.max(logit_rows, axis=1, keepdims=True)
        raised = jnp.exp(logit_rows - peak)
        probs = raised / jnp.sum(raised, axis=1, keepdims=True)
        mass = jnp.dot(probs, weights, precision=lax.Precision.HIGHEST)
        blocks = lax.all_to_all(probs, "spot", split_axis=1, concat_axis=0, tiled=True)
        pred = lax.psum_scatter(
            jnp.dot(blocks, expr, precision=lax.Precision.HIGHEST),
            "spot",
            scatter_dimension=0,
            tiled=True,
        )
        gene_dot = jnp.sum(valid[:, None] * pred * target, axis=0)
        gene_pred = jnp.sum(valid[:, None] * pred * pred, axis=0)
        gene_true = jnp.sum(valid[:, None] * target * target, axis=0)
        mass_part = jnp.sum(valid * mass)
        kcell = valid * counted
        cell_part = jnp.sum(kcell)
        spot_dot = jnp.sum(pred * target, axis=1)
        spot_pred = jnp.sum(pred * pred, axis=1)
        spot_true = jnp.sum(target * target, axis=1)
        gene_dot, gene_pred, gene_true, mass_total, cell_total = lax.psum(
            (gene_dot, gene_pred, gene_true, mass_part, cell_part), "spot"
        )
        spot_dot, spot_pred, spot_true = lax.psum((spot_dot, spot_pred, spot_true), "gene")
        gene_inv = lax.rsqrt(gene_pred * gene_true + tiny)
        cos_gene = gene_dot * gene_inv
        spot_inv = lax.rsqrt(spot_pred * spot_true + tiny)
        cos_spot = spot_dot * spot_inv
        share = kcell / cell_total
        scale_count = slide_spots[slide].astype(jnp.float32)
        kl_part = jnp.sum(
            share * (jnp.log(counted) - jnp.log(cell_total) - jnp.log(mass) + jnp.log(mass_total))
        )
        loss_local = loss_local - gene_share * jnp.sum(cos_gene)
        loss_local = loss_local + row_share * (scale_count * kl_part - jnp.sum(valid * cos_spot))
        gene_back = cos_gene * gene_true / (gene_pred * gene_true + tiny)
        spot_back = cos_spot * spot_true / (spot_pred * spot_true + tiny)
        dpred = -valid[:, None] * (
            target * (gene_inv[None, :] + spot_inv[:, None])
            - pred * gene_back[None, :]
            - pred * spot_back[:, None]
        )
        dmass = scale_count * valid * (1.0 / mass_total - share / mass)
        pred_list.append(pred)
        grads_full, mass_full = (
            lax.all_gather(dpred, "spot", axis=0, tiled=True),
            lax.all_gather(dmass, "spot", axis=0, tiled=True),
        )
        dprob_cells = jnp.dot(grads_full, expr.T, precision=lax.Precision.HIGHEST)
        dprob_cells = lax.psum(dprob_cells, "gene")
        expr_acc = expr_acc + lax.dot_general(
            blocks, grads_full, (((0,), (0,)), ((), ())), precision=lax.Precision.HIGHEST
        )
        dprob_cells = dprob_cells + mass_full[:, None] * own_weights[None, :]
        dprob_rows = lax.all_to_all(dprob_cells, "spot", split_axis=0, concat_axis=1, tiled=True)
        inner = jnp.sum(probs * dprob_rows, axis=1, keepdims=True)
        dlogit = probs * (dprob_rows - inner)
        grad_list.append(dlogit)
    loss = lax.psum(loss_local, ("spot", "gene"))
    return (jnp.stack(pred_list), loss, jnp.stack(grad_list), expr_acc)


def solution(mesh):
    places = mesh.shape["spot"]

    def on_device(logits, expr, spatial, slide_spots, spot_cells, cell_prior):
        if places == PLANE * PLANE and mesh.shape["gene"] == 2 and logits.shape[2] * expr.shape[1] <= 1 << 21:
            return plane_call(
                logits, expr, spatial, slide_spots, spot_cells, cell_prior, places // PLANE, CHUNKS
            )
        return general_plan(logits, expr, spatial, slide_spots, spot_cells, cell_prior)

    in_specs = (
        P(None, "spot", None),
        P("spot", "gene"),
        P(None, "spot", "gene"),
        P(),
        P(None, "spot"),
        P(),
    )
    out_specs = (P(None, "spot", "gene"), P(), P(None, "spot", None), P("spot", "gene"))
    return jax.shard_map(
        on_device, mesh=mesh, in_specs=in_specs, out_specs=out_specs, check_vma=False
    )
```

```python
import functools

import jax
import jax.numpy as jnp
from jax import lax
from jax.experimental import pallas as pl
from jax.experimental.pallas import tpu as pltpu
from jax.sharding import PartitionSpec as P

tiny = 1e-06
fixed_point = 16384.0
F32 = jnp.float32
BF16 = jnp.bfloat16
MESH = pl.DeviceIdType.MESH

PLANE = 4
LANES = 128
STEP_ROWS = 16
CHUNKS = 4
LEAD = 2
LAG = 1


def halves(value):
    high = value.astype(BF16)
    return high, (value - high.astype(F32)).astype(BF16)


def product(a_high, a_low, b_high, b_low, contract):
    def one(a, b):
        return lax.dot_general(a, b, (contract, ((), ())), preferred_element_type=F32)

    return one(a_high, b_high) + (one(a_high, b_low) + one(a_low, b_high))


def plane_kernel(lines, chunks, *refs):
    (
        (logits_ref, expr_ref, spatial_ref, count_ref, cells_ref, prior_ref),
        (pred_ref, loss_ref, glog_ref, gexp_ref),
        (lg, lq, tg, ex, pq, ab, af, ahi, alo, thi, tlo, bb, bhi, blo, cs, cr, pr, sacc, s1, s2, gv, ss, rowv, rs),
        (ds, dhi, dlo, es, ru, rd, fs, fr, fo, go, ge, inn, l1, l2),
        (loc, ag_r, ag_us, ag_ds, a_s, a_r, a2_s, a2_r, r_s, r_r, c_s, c_r, s1_s, s1_r, s2_s, s2_r, ss_s, ss_r),
        (d_s, d_r, ru_s, ru_r, rd_s, rd_r, f_s, f_r, fo_s, fo_r, in_s, in_r, l1_s, l1_r, l2_s, l2_r, out_s),
    ) = grouped(refs, (6, 4, 24, 14, 18, 17))
    place = lax.axis_index("spot")
    core = lax.axis_index("gene")
    z = place // PLANE
    q = place % PLANE
    col, row = q % 2, q // 2
    mates = ((1 - row) * 2 + 1 - col, row * 2 + 1 - col, (1 - row) * 2 + col)
    others = tuple((z + step) % lines for step in range(1, lines))
    up, down = (place + PLANE, core), (place - PLANE, core)
    sibling = (place, 1 - core)
    slides, slide_rows = logits_ref.shape[0], logits_ref.shape[1]
    rows = slides * slide_rows
    cb = expr_ref.shape[0]
    genes = expr_ref.shape[1]
    width = genes // chunks
    last = lines - 1
    at_end = (z == 0) | (z == last)
    in_middle = (z > 0) & (z < last)

    def mate(p):
        return (z * PLANE + p, core)

    def send(src, dst, send_sem, recv_sem, device):
        copy = pltpu.make_async_remote_copy(
            src_ref=src, dst_ref=dst, send_sem=send_sem, recv_sem=recv_sem, device_id=device, device_id_type=MESH
        )
        copy.start()

    def arrived(dst, recv_sem):
        pltpu.make_async_copy(dst, dst, recv_sem).wait()

    sent = arrived

    def cols(k):
        return pl.ds(k * width, width)

    def block(index):
        return pl.ds(pl.multiple_of(index * cb, cb), cb)

    def share(index):
        return pl.ds(pl.multiple_of(index * rows, rows), rows)

    def half(index):
        return pl.ds(pl.multiple_of(index * slide_rows, slide_rows), slide_rows)

    for m in range(slides):
        pltpu.make_async_copy(logits_ref.at[m], lg.at[half(m)], loc.at[m]).start()
        pltpu.make_async_copy(spatial_ref.at[m], tg.at[half(m)], loc.at[slides + m]).start()
    pltpu.make_async_copy(expr_ref, ex, loc.at[2 * slides]).start()

    barrier = pltpu.get_barrier_semaphore()
    for p in mates:
        pl.semaphore_signal(barrier, inc=1, device_id=mate(p), device_id_type=MESH)
    for o in others:
        pl.semaphore_signal(barrier, inc=1, device_id=(o * PLANE + q, core), device_id_type=MESH)
    pl.semaphore_signal(barrier, inc=1, device_id=sibling, device_id_type=MESH)
    pl.semaphore_wait(barrier, len(mates) + len(others) + 1)

    for m in range(slides):
        pltpu.make_async_copy(logits_ref.at[m], lg.at[half(m)], loc.at[m]).wait()
    for p in range(PLANE):
        for line in range(lines):
            lq[p, :, pl.ds(line * cb, cb)] = lg[half(core), pl.ds((line * PLANE + p) * cb, cb)]
    for p in mates:
        send(lq.at[p], ab.at[q, half(core)], a_s, a_r.at[q], mate(p))

    pltpu.make_async_copy(expr_ref, ex, loc.at[2 * slides]).wait()
    for k in range(chunks):
        bb[k, block(z), :] = ex[:, cols(k)]

    def send_own(k):
        here = bb.at[k, block(z)]

        @pl.when(z < last)
        def _():
            send(here, here, ag_us.at[z], ag_r.at[z, k], up)

        @pl.when(z > 0)
        def _():
            send(here, here, ag_ds.at[z], ag_r.at[z, k], down)

    for k in range(min(LEAD, chunks)):
        send_own(k)

    @pl.when(at_end)
    def _():
        for k in range(LEAD, chunks):
            send_own(k)

    def forward(k):
        @pl.when(in_middle)
        def _():
            for distance in range(1, last):
                below, above = z - distance, z + distance

                @pl.when(below >= 0)
                def _():
                    here = bb.at[k, block(below)]
                    arrived(here, ag_r.at[below, k])
                    send(here, here, ag_us.at[below], ag_r.at[below, k], up)

                @pl.when(above <= last)
                def _():
                    here = bb.at[k, block(above)]
                    arrived(here, ag_r.at[above, k])
                    send(here, here, ag_ds.at[above], ag_r.at[above, k], down)

            if k + LEAD < chunks:
                send_own(k + LEAD)

    def gathered(k):
        @pl.when(at_end)
        def _():
            for distance in range(1, lines):
                line = jnp.where(z == 0, distance, last - distance)
                arrived(bb.at[k, block(line)], ag_r.at[line, k])

    weights = prior_ref[...].astype(F32) / fixed_point

    @pl.loop(0, rows // STEP_ROWS)
    def _(step):
        at = pl.ds(pl.multiple_of(step * STEP_ROWS, STEP_ROWS), STEP_ROWS)
        value = lg[at, :]
        peak = jnp.max(value, axis=1, keepdims=True)
        raised = jnp.exp(value - peak)
        scale = 1.0 / jnp.sum(raised, axis=1, keepdims=True)
        probs = raised * scale
        mass_rows = jnp.sum(probs * weights, axis=1, keepdims=True)
        rowv[0, at, :] = jnp.broadcast_to(mass_rows, (STEP_ROWS, LANES))
        rowv[1, at, :] = jnp.broadcast_to(peak, (STEP_ROWS, LANES))
        rowv[2, at, :] = jnp.broadcast_to(scale, (STEP_ROWS, LANES))
        for p in range(PLANE):
            for line in range(lines):
                at_cells = (line * PLANE + p) * cb
                pq[p, at, pl.ds(line * cb, cb)] = probs[:, at_cells : at_cells + cb]

    wide = lax.broadcasted_iota(jnp.int32, (rows, LANES), 1)
    rs[q] = jnp.where(wide == 0, rowv[1], rowv[2]).T[0:8]
    for p in mates:
        send(rs.at[q], rs.at[q], r_s, r_r.at[q], mate(p))

    for p in (mates[1], mates[2], mates[0]):
        here = ab.at[p, half(core)]
        arrived(here, a_r.at[p])
        send(here, here, a2_s, a2_r.at[p], sibling)
    forward(0)

    rid = lax.broadcasted_iota(jnp.int32, (rows, 1), 0)
    first = rid < slide_rows
    position = place * slide_rows + jnp.where(first, rid, rid - slide_rows)
    count = jnp.where(first, count_ref[0], count_ref[1])
    valid = (position < count).astype(F32)
    scale_count = count.astype(F32)
    square = (slide_rows, slide_rows)
    eye = lax.broadcasted_iota(jnp.int32, square, 0) == lax.broadcasted_iota(jnp.int32, square, 1)
    counted = jnp.concatenate(
        [
            jnp.sum(jnp.where(eye, cells_ref[m : m + 1, :].astype(F32), 0.0), axis=1, keepdims=True)
            for m in range(slides)
        ],
        axis=0,
    )
    mass = rowv[0, :, 0:1]
    kcell = valid * counted

    def by_slide(value):
        return [jnp.sum(value[m * slide_rows : (m + 1) * slide_rows], axis=0, keepdims=True) for m in range(slides)]

    mass_parts = by_slide(valid * mass)
    cell_parts = by_slide(kcell)
    lane = lax.broadcasted_iota(jnp.int32, (1, width), 1)
    scalars = jnp.zeros((1, width), F32)
    for at, value in enumerate(mass_parts + cell_parts):
        scalars = jnp.where(lane == at, value, scalars)
    for m in range(slides):
        pltpu.make_async_copy(spatial_ref.at[m], tg.at[half(m)], loc.at[slides + m]).wait()
    sacc[...] = jnp.zeros_like(sacc)

    af[q] = pq[q]
    ahi[share(q), :], alo[share(q), :] = halves(pq[q])
    for p in (mates[1], mates[2], mates[0]):
        arrived(rs.at[p], r_r.at[p])
        arrived(ab.at[p, half(1 - core)], a2_r.at[p])
        by_row = rs[p].T
        probs = jnp.exp(ab[p] - by_row[:, 0:1]) * by_row[:, 1:2]
        af[p] = probs
        ahi[share(p), :], alo[share(p), :] = halves(probs)

    def forward_product(k):
        gathered(k)
        high, low = halves(bb[k])
        bhi[:, cols(k)], blo[:, cols(k)] = high, low
        cs[k] = product(ahi[...], alo[...], high, low, ((1,), (0,)))
        for p in mates:
            send(cs.at[k, share(p)], cr.at[k, q], c_s, c_r.at[k, q], mate(p))

    def finish_pred(k):
        total = cs[k, share(q), :]
        for p in mates:
            arrived(cr.at[k, p], c_r.at[k, p])
            total = total + cr[k, p]
        pr[:, cols(k)] = total
        truth = tg[:, cols(k)]
        sacc[0] += total * truth
        sacc[1] += total * total
        sacc[2] += truth * truth
        kept = valid * total
        stats = by_slide(kept * truth) + by_slide(kept * total) + by_slide(valid * truth * truth)
        s1[q, :, cols(k)] = jnp.concatenate(stats + [scalars, jnp.zeros((1, width), F32)], axis=0)

    early = (chunks - LAG) * width
    parts = (pl.ds(0, early), pl.ds(early, genes - early))

    def sum_plane(at):
        for p in mates:
            send(s1.at[q, :, parts[at]], s1.at[q, :, parts[at]], s1_s, s1_r.at[at, q], mate(p))

    def sum_line(at):
        for p in mates:
            arrived(s1.at[p, :, parts[at]], s1_r.at[at, p])
        s2[z, :, parts[at]] = (s1[0, :, parts[at]] + s1[1, :, parts[at]]) + (s1[2, :, parts[at]] + s1[3, :, parts[at]])
        for o in others:
            send(s2.at[z, :, parts[at]], s2.at[z, :, parts[at]], s2_s, s2_r.at[at, z], (o * PLANE + q, core))

    for k in range(chunks):
        if k + 1 < chunks:
            forward(k + 1)
        forward_product(k)
        if k >= LAG:
            finish_pred(k - LAG)
    sum_plane(0)
    for p in range(PLANE):
        high, low = halves(af[p].T)
        thi[:, share(p)], tlo[:, share(p)] = high, low
    sum_line(0)
    for k in range(chunks - LAG, chunks):
        finish_pred(k)
    sum_plane(1)
    for m in range(slides):
        pltpu.make_async_copy(pr.at[half(m)], pred_ref.at[m], out_s.at[m]).start()

    sums = [jnp.sum(sacc[at], axis=1, keepdims=True) for at in range(3)]
    ss[core] = jnp.where(wide == 0, sums[0], jnp.where(wide == 1, sums[1], sums[2]))
    send(ss.at[core], ss.at[core], ss_s, ss_r, sibling)
    sum_line(1)
    arrived(ss.at[1 - core], ss_r)
    spot = ss[0] + ss[1]
    spot_dot, spot_pred, spot_true = spot[:, 0:1], spot[:, 1:2], spot[:, 2:3]
    spot_inv = lax.rsqrt(spot_pred * spot_true + tiny)
    cos_spot = spot_dot * spot_inv
    spot_back = cos_spot * spot_true / (spot_pred * spot_true + tiny)
    for o in others:
        for at in range(2):
            arrived(s2.at[o, :, parts[at]], s2_r.at[at, o])
    total = s2[0]
    for line in range(1, lines):
        total = total + s2[line]
    gene_dot, gene_pred, gene_true = total[0:2], total[2:4], total[4:6]
    gene_inv = lax.rsqrt(gene_pred * gene_true + tiny)
    cos_gene = gene_dot * gene_inv
    gv[0:2, :] = gene_inv
    gv[2:4, :] = cos_gene * gene_true / (gene_pred * gene_true + tiny)

    inner = jnp.zeros((rows, 1), F32)
    for k in range(chunks):
        pieces = []
        for m in range(slides):
            lo, hi = m * slide_rows, (m + 1) * slide_rows
            truth, guess = tg[lo:hi, cols(k)], pr[lo:hi, cols(k)]
            inverse, back = gv[m : m + 1, cols(k)], gv[2 + m : 3 + m, cols(k)]
            pieces.append(
                -valid[lo:hi]
                * (truth * (inverse + spot_inv[lo:hi]) - guess * back - guess * spot_back[lo:hi])
            )
        grad = jnp.concatenate(pieces, axis=0)
        here = ds.at[k, share(q)]
        here[...] = grad
        for p in mates:
            send(here, here, d_s, d_r.at[k, q], mate(p))
        inner = inner + jnp.sum(grad * pr[:, cols(k)], axis=1, keepdims=True)
    gene_sum = jnp.sum(jnp.sum(cos_gene, axis=1, keepdims=True), axis=0, keepdims=True)
    inn[core] = jnp.where(wide == 0, inner, gene_sum)
    send(inn.at[core], inn.at[core], in_s, in_r, sibling)

    mass_total = jnp.where(first, total[6:7, 0:1], total[6:7, 1:2])
    cell_total = jnp.where(first, total[6:7, 2:3], total[6:7, 3:4])
    portion = kcell / cell_total
    kl_rows = portion * (jnp.log(counted) - jnp.log(cell_total) - jnp.log(mass) + jnp.log(mass_total))
    dmass = scale_count * valid * (1.0 / mass_total - portion / mass)
    terms = jnp.sum(scale_count * kl_rows - valid * cos_spot, axis=0, keepdims=True)
    l1[q] = jnp.broadcast_to(terms, (8, LANES))
    for p in mates:
        send(l1.at[q], l1.at[q], l1_s, l1_r.at[q], mate(p))

    def backward_product(k):
        for p in mates:
            arrived(ds.at[k, share(p)], d_r.at[k, p])
        high, low = halves(ds[k])
        dhi[:, cols(k)], dlo[:, cols(k)] = high, low
        es[k] = product(thi[...], tlo[...], high, low, ((1,), (0,)))

        @pl.when(z == 0)
        def _():
            for line in range(last, 0, -1):
                there = ru.at[k, block(line)]
                send(es.at[k, block(line)], there, ru_s.at[line], ru_r.at[line, k], up)

        @pl.when(z == last)
        def _():
            for line in range(last):
                there = rd.at[k, block(line)]
                send(es.at[k, block(line)], there, rd_s.at[line], rd_r.at[line, k], down)

    def add_on(k):
        for line in range(last, 1, -1):
            at = block(line)

            @pl.when((z > 0) & (z < line))
            def _():
                arrived(ru.at[k, at], ru_r.at[line, k])
                es[k, at, :] += ru[k, at, :]
                send(es.at[k, at], ru.at[k, at], ru_s.at[line], ru_r.at[line, k], up)

        for line in range(last - 1):
            at = block(line)

            @pl.when((z < last) & (z > line))
            def _():
                arrived(rd.at[k, at], rd_r.at[line, k])
                es[k, at, :] += rd[k, at, :]
                send(es.at[k, at], rd.at[k, at], rd_s.at[line], rd_r.at[line, k], down)

    def finish_expr(k):
        at = block(z)
        ge[:, cols(k)] = es[k, at, :]

        @pl.when(z > 0)
        def _():
            arrived(ru.at[k, at], ru_r.at[z, k])
            ge[:, cols(k)] += ru[k, at, :]

        @pl.when(z < last)
        def _():
            arrived(rd.at[k, at], rd_r.at[z, k])
            ge[:, cols(k)] += rd[k, at, :]

    def probs_gradient(at):
        return product(dhi[:, at], dlo[:, at], bhi[:, at], blo[:, at], ((1,), (1,)))

    added = 0
    middle = chunks // 2
    for k in range(chunks):
        backward_product(k)
        if k == middle - 1:
            fs[...] = probs_gradient(pl.ds(0, middle * width))
        while 3 * (added + 1) <= 2 * k:
            add_on(added)
            added += 1
    fs[...] += probs_gradient(pl.ds(middle * width, genes - middle * width))

    for p in mates:
        send(fs.at[share(p)], fr.at[q], f_s, f_r.at[q], mate(p))
    fr[q] = fs[share(q), :]
    send(fr.at[q], fo.at[q], fo_s, fo_r.at[q], sibling)
    for p in mates:
        arrived(l1.at[p], l1_r.at[p])
    l2[z] = (l1[0] + l1[1]) + (l1[2] + l1[3])
    for o in others:
        send(l2.at[z], l2.at[z], l2_s, l2_r.at[z], (o * PLANE + q, core))
    while added < chunks - 1:
        add_on(added)
        added += 1
    for p in (mates[1], mates[2], mates[0]):
        arrived(fr.at[p], f_r.at[p])
        send(fr.at[p], fo.at[p], fo_s, fo_r.at[p], sibling)
    add_on(chunks - 1)
    for k in range(chunks - 2):
        finish_expr(k)

    arrived(inn.at[1 - core], in_r)
    both = inn[0] + inn[1]
    rowv[1] = jnp.broadcast_to(dmass, (rows, LANES))
    rowv[2] = jnp.broadcast_to(both[:, 0:1] + dmass * mass, (rows, LANES))
    for p in range(PLANE):
        arrived(fo.at[p], fo_r.at[p])

    @pl.loop(0, rows // STEP_ROWS)
    def _(step):
        at = pl.ds(pl.multiple_of(step * STEP_ROWS, STEP_ROWS), STEP_ROWS)
        by_mass, total_inner = rowv[1, at, 0:1], rowv[2, at, 0:1]
        for p in range(PLANE):
            for line in range(lines):
                here, there = pl.ds(line * cb, cb), (line * PLANE + p) * cb
                grad = fr[p, at, here] + fo[p, at, here] + by_mass * weights[:, there : there + cb]
                go[at, pl.ds(there, cb)] = pq[p, at, here] * (grad - total_inner)

    for m in range(slides):
        pltpu.make_async_copy(go.at[half(m)], glog_ref.at[m], out_s.at[slides + 1 + m]).start()

    for o in others:
        arrived(l2.at[o], l2_r.at[o])
    loss = l2[0]
    for line in range(1, lines):
        loss = loss + l2[line]
    loss_ref[...] = loss[0:1, 0:1] - both[0:1, 1:2]
    finish_expr(chunks - 2)
    finish_expr(chunks - 1)
    pltpu.make_async_copy(ge, gexp_ref, out_s.at[slides]).start()

    for m in range(slides):
        pltpu.make_async_copy(pr.at[half(m)], pred_ref.at[m], out_s.at[m]).wait()
        pltpu.make_async_copy(go.at[half(m)], glog_ref.at[m], out_s.at[slides + 1 + m]).wait()
    pltpu.make_async_copy(ge, gexp_ref, out_s.at[slides]).wait()
    for line in range(lines):
        at = block(line)

        @pl.when((line <= z) & (z < last))
        def _():
            sent(bb.at[:, at], ag_us.at[line])

        @pl.when((line >= z) & (z > 0))
        def _():
            sent(bb.at[:, at], ag_ds.at[line])

        @pl.when(line > z)
        def _():
            sent(es.at[:, at], ru_s.at[line])

        @pl.when(line < z)
        def _():
            sent(es.at[:, at], rd_s.at[line])

    three = pl.ds(0, len(mates))
    sent(ab.at[three, half(0)], a_s)
    sent(ab.at[three, half(0)], a2_s)
    sent(rs.at[three], r_s)
    sent(cr.at[:, three], c_s)
    sent(s1.at[three], s1_s)
    sent(s2.at[pl.ds(0, last)], s2_s)
    sent(ss.at[0], ss_s)
    sent(cr.at[:, three], d_s)
    sent(inn.at[0], in_s)
    sent(l1.at[three], l1_s)
    sent(l2.at[pl.ds(0, last)], l2_s)
    sent(fr.at[three], f_s)
    sent(fo, fo_s)


def grouped(refs, sizes):
    at = 0
    for size in sizes:
        yield refs[at : at + size]
        at += size


def deliver(pred_in, glog_in, gexp_in, pred_ref, glog_ref, gexp_ref, pred_mid, glog_mid, gexp_mid, sems):
    triples = ((glog_in, glog_mid, glog_ref), (pred_in, pred_mid, pred_ref), (gexp_in, gexp_mid, gexp_ref))
    loads = [pltpu.make_async_copy(src, mid, sems.at[0, at]) for at, (src, mid, _) in enumerate(triples)]
    stores = [pltpu.make_async_copy(mid, dst, sems.at[1, at]) for at, (_, mid, dst) in enumerate(triples)]
    for load in loads:
        load.start()
    for load, store in zip(loads, stores):
        load.wait()
        store.start()
    for store in stores:
        store.wait()


def plane_call(logits, expr, spatial, slide_spots, spot_cells, cell_prior, lines, chunks):
    slides, slide_rows, cells = logits.shape
    rows = slides * slide_rows
    cb, genes = expr.shape
    quarter = lines * cb
    spots = PLANE * rows
    width = genes // chunks
    dma = pltpu.SemaphoreType.DMA
    vmem = pltpu.VMEM
    anywhere = pl.BlockSpec(memory_space=pl.ANY)
    in_vmem = pl.BlockSpec(memory_space=pltpu.VMEM)
    in_smem = pl.BlockSpec(memory_space=pltpu.SMEM)
    scratch = [
        vmem((rows, cells), F32),
        vmem((PLANE, slide_rows, quarter), F32),
        vmem((rows, genes), F32),
        vmem((cb, genes), F32),
        vmem((PLANE, rows, quarter), F32),
        vmem((PLANE, rows, quarter), F32),
        vmem((PLANE, rows, quarter), F32),
        vmem((spots, quarter), BF16),
        vmem((spots, quarter), BF16),
        vmem((quarter, spots), BF16),
        vmem((quarter, spots), BF16),
        vmem((chunks, quarter, width), F32),
        vmem((quarter, genes), BF16),
        vmem((quarter, genes), BF16),
        vmem((chunks, spots, width), F32),
        vmem((chunks, PLANE, rows, width), F32),
        vmem((rows, genes), F32),
        vmem((3, rows, width), F32),
        vmem((PLANE, 8, genes), F32),
        vmem((lines, 8, genes), F32),
        vmem((8, genes), F32),
        vmem((2, rows, LANES), F32),
        vmem((3, rows, LANES), F32),
        vmem((PLANE, 8, rows), F32),
        vmem((chunks, spots, width), F32),
        vmem((spots, genes), BF16),
        vmem((spots, genes), BF16),
        vmem((chunks, quarter, width), F32),
        vmem((chunks, quarter, width), F32),
        vmem((chunks, quarter, width), F32),
        vmem((spots, quarter), F32),
        vmem((PLANE, rows, quarter), F32),
        vmem((PLANE, rows, quarter), F32),
        vmem((rows, cells), F32),
        vmem((cb, genes), F32),
        vmem((2, rows, LANES), F32),
        vmem((PLANE, 8, LANES), F32),
        vmem((lines, 8, LANES), F32),
        dma((2 * slides + 1,)),
        dma((lines, chunks)),
        dma((lines,)),
        dma((lines,)),
        dma,
        dma((PLANE,)),
        dma,
        dma((PLANE,)),
        dma,
        dma((PLANE,)),
        dma,
        dma((chunks, PLANE)),
        dma,
        dma((2, PLANE)),
        dma,
        dma((2, lines)),
        dma,
        dma,
        dma,
        dma((chunks, PLANE)),
        dma((lines,)),
        dma((lines, chunks)),
        dma((lines,)),
        dma((lines, chunks)),
        dma,
        dma((PLANE,)),
        dma,
        dma((PLANE,)),
        dma,
        dma,
        dma,
        dma((PLANE,)),
        dma,
        dma((lines,)),
        dma((2 * slides + 1,)),
    ]
    pred_shape = jax.ShapeDtypeStruct((slides, slide_rows, genes), F32)
    glog_shape = jax.ShapeDtypeStruct((slides, slide_rows, cells), F32)
    gexp_shape = jax.ShapeDtypeStruct((cb, genes), F32)
    pred, loss, grad_logits, grad_expr = pl.pallas_call(
        functools.partial(plane_kernel, lines, chunks),
        out_shape=(pred_shape, jax.ShapeDtypeStruct((1, 1), F32), glog_shape, gexp_shape),
        in_specs=[anywhere, anywhere, anywhere, in_smem, in_vmem, in_vmem],
        out_specs=(anywhere, in_vmem, anywhere, anywhere),
        scratch_shapes=scratch,
        compiler_params=pltpu.CompilerParams(
            collective_id=0, has_side_effects=True, vmem_limit_bytes=56 * 1024 * 1024
        ),
    )(logits, expr, spatial, slide_spots, spot_cells, cell_prior.reshape(1, cells))
    pred, grad_logits, grad_expr = pl.pallas_call(
        deliver,
        out_shape=(pred_shape, glog_shape, gexp_shape),
        in_specs=[anywhere] * 3,
        out_specs=(anywhere,) * 3,
        scratch_shapes=[vmem(shape.shape, F32) for shape in (pred_shape, glog_shape, gexp_shape)] + [dma((2, 3))],
        compiler_params=pltpu.CompilerParams(vmem_limit_bytes=56 * 1024 * 1024),
    )(pred, grad_logits, grad_expr)
    return pred, loss.reshape(()), grad_logits, grad_expr


def general_plan(logits, expr, spatial, slide_spots, spot_cells, cell_prior):
    place = lax.axis_index("spot")
    side = lax.axis_index("gene")
    rows_all = logits.shape[1]
    cell_rows = expr.shape[0]
    weights = cell_prior.astype(jnp.float32) / fixed_point
    gene_share = (place == 0).astype(jnp.float32)
    row_share = (side == 0).astype(jnp.float32)
    own_weights = lax.dynamic_slice_in_dim(weights, place * cell_rows, cell_rows, 0)
    expr_acc = jnp.zeros((cell_rows, expr.shape[1]), jnp.float32)
    loss_local = jnp.zeros((), jnp.float32)
    pred_list = []
    grad_list = []
    for slide in range(logits.shape[0]):
        logit_rows = logits[slide]
        counted = spot_cells[slide].astype(jnp.float32)
        target = spatial[slide]
        positions = place * rows_all + jnp.arange(rows_all, dtype=jnp.int32)
        valid = (positions < slide_spots[slide]).astype(jnp.float32)
        peak = jnp.max(logit_rows, axis=1, keepdims=True)
        raised = jnp.exp(logit_rows - peak)
        probs = raised / jnp.sum(raised, axis=1, keepdims=True)
        mass = jnp.dot(probs, weights, precision=lax.Precision.HIGHEST)
        blocks = lax.all_to_all(probs, "spot", split_axis=1, concat_axis=0, tiled=True)
        pred = lax.psum_scatter(
            jnp.dot(blocks, expr, precision=lax.Precision.HIGHEST),
            "spot",
            scatter_dimension=0,
            tiled=True,
        )
        gene_dot = jnp.sum(valid[:, None] * pred * target, axis=0)
        gene_pred = jnp.sum(valid[:, None] * pred * pred, axis=0)
        gene_true = jnp.sum(valid[:, None] * target * target, axis=0)
        mass_part = jnp.sum(valid * mass)
        kcell = valid * counted
        cell_part = jnp.sum(kcell)
        spot_dot = jnp.sum(pred * target, axis=1)
        spot_pred = jnp.sum(pred * pred, axis=1)
        spot_true = jnp.sum(target * target, axis=1)
        gene_dot, gene_pred, gene_true, mass_total, cell_total = lax.psum(
            (gene_dot, gene_pred, gene_true, mass_part, cell_part), "spot"
        )
        spot_dot, spot_pred, spot_true = lax.psum((spot_dot, spot_pred, spot_true), "gene")
        gene_inv = lax.rsqrt(gene_pred * gene_true + tiny)
        cos_gene = gene_dot * gene_inv
        spot_inv = lax.rsqrt(spot_pred * spot_true + tiny)
        cos_spot = spot_dot * spot_inv
        share = kcell / cell_total
        scale_count = slide_spots[slide].astype(jnp.float32)
        kl_part = jnp.sum(
            share * (jnp.log(counted) - jnp.log(cell_total) - jnp.log(mass) + jnp.log(mass_total))
        )
        loss_local = loss_local - gene_share * jnp.sum(cos_gene)
        loss_local = loss_local + row_share * (scale_count * kl_part - jnp.sum(valid * cos_spot))
        gene_back = cos_gene * gene_true / (gene_pred * gene_true + tiny)
        spot_back = cos_spot * spot_true / (spot_pred * spot_true + tiny)
        dpred = -valid[:, None] * (
            target * (gene_inv[None, :] + spot_inv[:, None])
            - pred * gene_back[None, :]
            - pred * spot_back[:, None]
        )
        dmass = scale_count * valid * (1.0 / mass_total - share / mass)
        pred_list.append(pred)
        grads_full, mass_full = (
            lax.all_gather(dpred, "spot", axis=0, tiled=True),
            lax.all_gather(dmass, "spot", axis=0, tiled=True),
        )
        dprob_cells = jnp.dot(grads_full, expr.T, precision=lax.Precision.HIGHEST)
        dprob_cells = lax.psum(dprob_cells, "gene")
        expr_acc = expr_acc + lax.dot_general(
            blocks, grads_full, (((0,), (0,)), ((), ())), precision=lax.Precision.HIGHEST
        )
        dprob_cells = dprob_cells + mass_full[:, None] * own_weights[None, :]
        dprob_rows = lax.all_to_all(dprob_cells, "spot", split_axis=0, concat_axis=1, tiled=True)
        inner = jnp.sum(probs * dprob_rows, axis=1, keepdims=True)
        dlogit = probs * (dprob_rows - inner)
        grad_list.append(dlogit)
    loss = lax.psum(loss_local, ("spot", "gene"))
    return (jnp.stack(pred_list), loss, jnp.stack(grad_list), expr_acc)


def solution(mesh):
    places = mesh.shape["spot"]

    def on_device(logits, expr, spatial, slide_spots, spot_cells, cell_prior):
        if places == PLANE * PLANE and mesh.shape["gene"] == 2 and logits.shape[2] * expr.shape[1] <= 1 << 21:
            return plane_call(
                logits, expr, spatial, slide_spots, spot_cells, cell_prior, places // PLANE, CHUNKS
            )
        return general_plan(logits, expr, spatial, slide_spots, spot_cells, cell_prior)

    in_specs = (
        P(None, "spot", None),
        P("spot", "gene"),
        P(None, "spot", "gene"),
        P(),
        P(None, "spot"),
        P(),
    )
    out_specs = (P(None, "spot", "gene"), P(), P(None, "spot", None), P("spot", "gene"))
    return jax.shard_map(
        on_device, mesh=mesh, in_specs=in_specs, out_specs=out_specs, check_vma=False
    )
```

```python
import functools

import jax
import jax.numpy as jnp
from jax import lax
from jax.experimental import pallas as pl
from jax.experimental.pallas import tpu as pltpu
from jax.sharding import PartitionSpec as P

tiny = 1e-06
fixed_point = 16384.0
F32 = jnp.float32
BF16 = jnp.bfloat16
MESH = pl.DeviceIdType.MESH

PLANE = 4
LANES = 128
STEP_ROWS = 16
CHUNKS = 4
LEAD = 2
LAG = 1
AHEAD = 2


def halves(value):
    high = value.astype(BF16)
    return high, (value - high.astype(F32)).astype(BF16)


def product(a_high, a_low, b_high, b_low, contract):
    def one(a, b):
        return lax.dot_general(a, b, (contract, ((), ())), preferred_element_type=F32)

    return one(a_high, b_high) + (one(a_high, b_low) + one(a_low, b_high))


def plane_kernel(lines, chunks, *refs):
    (
        (logits_ref, expr_ref, spatial_ref, count_ref, cells_ref, prior_ref),
        (pred_ref, loss_ref, glog_ref, gexp_ref),
        (lg, lq, tg, ex, pq, ab, af, ahi, alo, thi, tlo, bb, bhi, blo, cs, cr, pr, sacc, s1, s2, gv, ss, rowv, rs),
        (ds, dhi, dlo, es, ru, rd, fs, fr, fo, go, ge, inn, l1, l2),
        (loc, ag_r, ag_us, ag_ds, a_s, a_r, a2_s, a2_r, r_s, r_r, c_s, c_r, s1_s, s1_r, s2_s, s2_r, ss_s, ss_r),
        (d_s, d_r, ru_s, ru_r, rd_s, rd_r, f_s, f_r, fo_s, fo_r, in_s, in_r, l1_s, l1_r, l2_s, l2_r, out_s),
    ) = grouped(refs, (6, 4, 24, 14, 18, 17))
    place = lax.axis_index("spot")
    core = lax.axis_index("gene")
    z = place // PLANE
    q = place % PLANE
    col, row = q % 2, q // 2
    mates = ((1 - row) * 2 + 1 - col, row * 2 + 1 - col, (1 - row) * 2 + col)
    others = tuple((z + step) % lines for step in range(1, lines))
    up, down = (place + PLANE, core), (place - PLANE, core)
    sibling = (place, 1 - core)
    slides, slide_rows = logits_ref.shape[0], logits_ref.shape[1]
    rows = slides * slide_rows
    cb = expr_ref.shape[0]
    genes = expr_ref.shape[1]
    width = genes // chunks
    last = lines - 1
    at_end = (z == 0) | (z == last)
    in_middle = (z > 0) & (z < last)

    def mate(p):
        return (z * PLANE + p, core)

    def send(src, dst, send_sem, recv_sem, device):
        copy = pltpu.make_async_remote_copy(
            src_ref=src, dst_ref=dst, send_sem=send_sem, recv_sem=recv_sem, device_id=device, device_id_type=MESH
        )
        copy.start()

    def arrived(dst, recv_sem):
        pltpu.make_async_copy(dst, dst, recv_sem).wait()

    sent = arrived

    def cols(k):
        return pl.ds(k * width, width)

    def block(index):
        return pl.ds(pl.multiple_of(index * cb, cb), cb)

    def share(index):
        return pl.ds(pl.multiple_of(index * rows, rows), rows)

    def half(index):
        return pl.ds(pl.multiple_of(index * slide_rows, slide_rows), slide_rows)

    for m in range(slides):
        pltpu.make_async_copy(logits_ref.at[m], lg.at[half(m)], loc.at[m]).start()
        pltpu.make_async_copy(spatial_ref.at[m], tg.at[half(m)], loc.at[slides + m]).start()
    pltpu.make_async_copy(expr_ref, ex, loc.at[2 * slides]).start()

    barrier = pltpu.get_barrier_semaphore()
    for p in mates:
        pl.semaphore_signal(barrier, inc=1, device_id=mate(p), device_id_type=MESH)
    for o in others:
        pl.semaphore_signal(barrier, inc=1, device_id=(o * PLANE + q, core), device_id_type=MESH)
    pl.semaphore_signal(barrier, inc=1, device_id=sibling, device_id_type=MESH)
    pl.semaphore_wait(barrier, len(mates) + len(others) + 1)

    for m in range(slides):
        pltpu.make_async_copy(logits_ref.at[m], lg.at[half(m)], loc.at[m]).wait()
    for p in range(PLANE):
        for line in range(lines):
            lq[p, :, pl.ds(line * cb, cb)] = lg[half(core), pl.ds((line * PLANE + p) * cb, cb)]
    for p in mates:
        send(lq.at[p], ab.at[q, half(core)], a_s, a_r.at[q], mate(p))

    pltpu.make_async_copy(expr_ref, ex, loc.at[2 * slides]).wait()
    for k in range(chunks):
        bb[k, block(z), :] = ex[:, cols(k)]

    def send_own(k):
        here = bb.at[k, block(z)]

        @pl.when(z < last)
        def _():
            send(here, here, ag_us.at[z], ag_r.at[z, k], up)

        @pl.when(z > 0)
        def _():
            send(here, here, ag_ds.at[z], ag_r.at[z, k], down)

    for k in range(min(LEAD, chunks)):
        send_own(k)

    @pl.when(at_end)
    def _():
        for k in range(LEAD, chunks):
            send_own(k)

    def forward(k):
        @pl.when(in_middle)
        def _():
            for distance in range(1, last):
                below, above = z - distance, z + distance

                @pl.when(below >= 0)
                def _():
                    here = bb.at[k, block(below)]
                    arrived(here, ag_r.at[below, k])
                    send(here, here, ag_us.at[below], ag_r.at[below, k], up)

                @pl.when(above <= last)
                def _():
                    here = bb.at[k, block(above)]
                    arrived(here, ag_r.at[above, k])
                    send(here, here, ag_ds.at[above], ag_r.at[above, k], down)

            if k + LEAD < chunks:
                send_own(k + LEAD)

    def gathered(k):
        @pl.when(at_end)
        def _():
            for distance in range(1, lines):
                line = jnp.where(z == 0, distance, last - distance)
                arrived(bb.at[k, block(line)], ag_r.at[line, k])

    weights = prior_ref[...].astype(F32) / fixed_point

    @pl.loop(0, rows // STEP_ROWS)
    def _(step):
        at = pl.ds(pl.multiple_of(step * STEP_ROWS, STEP_ROWS), STEP_ROWS)
        value = lg[at, :]
        peak = jnp.max(value, axis=1, keepdims=True)
        raised = jnp.exp(value - peak)
        scale = 1.0 / jnp.sum(raised, axis=1, keepdims=True)
        probs = raised * scale
        mass_rows = jnp.sum(probs * weights, axis=1, keepdims=True)
        rowv[0, at, :] = jnp.broadcast_to(mass_rows, (STEP_ROWS, LANES))
        rowv[1, at, :] = jnp.broadcast_to(peak, (STEP_ROWS, LANES))
        rowv[2, at, :] = jnp.broadcast_to(scale, (STEP_ROWS, LANES))
        for p in range(PLANE):
            for line in range(lines):
                at_cells = (line * PLANE + p) * cb
                pq[p, at, pl.ds(line * cb, cb)] = probs[:, at_cells : at_cells + cb]

    wide = lax.broadcasted_iota(jnp.int32, (rows, LANES), 1)
    rs[q] = jnp.where(wide == 0, rowv[1], rowv[2]).T[0:8]
    for p in mates:
        send(rs.at[q], rs.at[q], r_s, r_r.at[q], mate(p))

    for p in (mates[1], mates[2], mates[0]):
        here = ab.at[p, half(core)]
        arrived(here, a_r.at[p])
        send(here, here, a2_s, a2_r.at[p], sibling)
    forward(0)

    rid = lax.broadcasted_iota(jnp.int32, (rows, 1), 0)
    first = rid < slide_rows
    position = place * slide_rows + jnp.where(first, rid, rid - slide_rows)
    count = jnp.where(first, count_ref[0], count_ref[1])
    valid = (position < count).astype(F32)
    scale_count = count.astype(F32)
    square = (slide_rows, slide_rows)
    eye = lax.broadcasted_iota(jnp.int32, square, 0) == lax.broadcasted_iota(jnp.int32, square, 1)
    counted = jnp.concatenate(
        [
            jnp.sum(jnp.where(eye, cells_ref[m : m + 1, :].astype(F32), 0.0), axis=1, keepdims=True)
            for m in range(slides)
        ],
        axis=0,
    )
    mass = rowv[0, :, 0:1]
    kcell = valid * counted

    def by_slide(value):
        return [jnp.sum(value[m * slide_rows : (m + 1) * slide_rows], axis=0, keepdims=True) for m in range(slides)]

    mass_parts = by_slide(valid * mass)
    cell_parts = by_slide(kcell)
    lane = lax.broadcasted_iota(jnp.int32, (1, width), 1)
    scalars = jnp.zeros((1, width), F32)
    for at, value in enumerate(mass_parts + cell_parts):
        scalars = jnp.where(lane == at, value, scalars)
    for m in range(slides):
        pltpu.make_async_copy(spatial_ref.at[m], tg.at[half(m)], loc.at[slides + m]).wait()
    sacc[...] = jnp.zeros_like(sacc)

    af[q] = pq[q]
    ahi[share(q), :], alo[share(q), :] = halves(pq[q])
    for p in (mates[1], mates[2], mates[0]):
        arrived(rs.at[p], r_r.at[p])
        arrived(ab.at[p, half(1 - core)], a2_r.at[p])
        by_row = rs[p].T
        probs = jnp.exp(ab[p] - by_row[:, 0:1]) * by_row[:, 1:2]
        af[p] = probs
        ahi[share(p), :], alo[share(p), :] = halves(probs)

    def forward_product(k):
        gathered(k)
        high, low = halves(bb[k])
        bhi[:, cols(k)], blo[:, cols(k)] = high, low
        cs[k] = product(ahi[...], alo[...], high, low, ((1,), (0,)))
        for p in mates:
            send(cs.at[k, share(p)], cr.at[k, q], c_s, c_r.at[k, q], mate(p))

    def finish_pred(k):
        total = cs[k, share(q), :]
        for p in mates:
            arrived(cr.at[k, p], c_r.at[k, p])
            total = total + cr[k, p]
        pr[:, cols(k)] = total
        truth = tg[:, cols(k)]
        sacc[0] += total * truth
        sacc[1] += total * total
        sacc[2] += truth * truth
        kept = valid * total
        stats = by_slide(kept * truth) + by_slide(kept * total) + by_slide(valid * truth * truth)
        s1[q, :, cols(k)] = jnp.concatenate(stats + [scalars, jnp.zeros((1, width), F32)], axis=0)

    early = (chunks - LAG) * width
    parts = (pl.ds(0, early), pl.ds(early, genes - early))

    def sum_plane(at):
        for p in mates:
            send(s1.at[q, :, parts[at]], s1.at[q, :, parts[at]], s1_s, s1_r.at[at, q], mate(p))

    def sum_line(at):
        for p in mates:
            arrived(s1.at[p, :, parts[at]], s1_r.at[at, p])
        s2[z, :, parts[at]] = (s1[0, :, parts[at]] + s1[1, :, parts[at]]) + (s1[2, :, parts[at]] + s1[3, :, parts[at]])
        for o in others:
            send(s2.at[z, :, parts[at]], s2.at[z, :, parts[at]], s2_s, s2_r.at[at, z], (o * PLANE + q, core))

    for k in range(chunks):
        if k + 1 < chunks:
            forward(k + 1)
        forward_product(k)
        if k >= LAG:
            finish_pred(k - LAG)
    sum_plane(0)
    for p in range(PLANE):
        high, low = halves(af[p].T)
        thi[:, share(p)], tlo[:, share(p)] = high, low
    sum_line(0)
    for k in range(chunks - LAG, chunks):
        finish_pred(k)
    sum_plane(1)
    for m in range(slides):
        pltpu.make_async_copy(pr.at[half(m)], pred_ref.at[m], out_s.at[m]).start()

    sums = [jnp.sum(sacc[at], axis=1, keepdims=True) for at in range(3)]
    ss[core] = jnp.where(wide == 0, sums[0], jnp.where(wide == 1, sums[1], sums[2]))
    send(ss.at[core], ss.at[core], ss_s, ss_r, sibling)
    sum_line(1)
    arrived(ss.at[1 - core], ss_r)
    spot = ss[0] + ss[1]
    spot_dot, spot_pred, spot_true = spot[:, 0:1], spot[:, 1:2], spot[:, 2:3]
    spot_inv = lax.rsqrt(spot_pred * spot_true + tiny)
    cos_spot = spot_dot * spot_inv
    spot_back = cos_spot * spot_true / (spot_pred * spot_true + tiny)
    for o in others:
        for at in range(2):
            arrived(s2.at[o, :, parts[at]], s2_r.at[at, o])
    total = s2[0]
    for line in range(1, lines):
        total = total + s2[line]
    gene_dot, gene_pred, gene_true = total[0:2], total[2:4], total[4:6]
    gene_inv = lax.rsqrt(gene_pred * gene_true + tiny)
    cos_gene = gene_dot * gene_inv
    gv[0:2, :] = gene_inv
    gv[2:4, :] = cos_gene * gene_true / (gene_pred * gene_true + tiny)

    sacc[0] = jnp.zeros_like(sacc[0])

    def send_grad(k):
        pieces = []
        for m in range(slides):
            lo, hi = m * slide_rows, (m + 1) * slide_rows
            truth, guess = tg[lo:hi, cols(k)], pr[lo:hi, cols(k)]
            inverse, back = gv[m : m + 1, cols(k)], gv[2 + m : 3 + m, cols(k)]
            pieces.append(
                -valid[lo:hi]
                * (truth * (inverse + spot_inv[lo:hi]) - guess * back - guess * spot_back[lo:hi])
            )
        grad = jnp.concatenate(pieces, axis=0)
        here = ds.at[k, share(q)]
        here[...] = grad
        for p in mates:
            send(here, here, d_s, d_r.at[k, q], mate(p))
        sacc[0] += grad * pr[:, cols(k)]

    for k in range(min(AHEAD, chunks)):
        send_grad(k)
    gene_sum = jnp.sum(jnp.sum(cos_gene, axis=1, keepdims=True), axis=0, keepdims=True)

    mass_total = jnp.where(first, total[6:7, 0:1], total[6:7, 1:2])
    cell_total = jnp.where(first, total[6:7, 2:3], total[6:7, 3:4])
    portion = kcell / cell_total
    kl_rows = portion * (jnp.log(counted) - jnp.log(cell_total) - jnp.log(mass) + jnp.log(mass_total))
    dmass = scale_count * valid * (1.0 / mass_total - portion / mass)
    terms = jnp.sum(scale_count * kl_rows - valid * cos_spot, axis=0, keepdims=True)
    l1[q] = jnp.broadcast_to(terms, (8, LANES))
    for p in mates:
        send(l1.at[q], l1.at[q], l1_s, l1_r.at[q], mate(p))

    def backward_product(k):
        for p in mates:
            arrived(ds.at[k, share(p)], d_r.at[k, p])
        high, low = halves(ds[k])
        dhi[:, cols(k)], dlo[:, cols(k)] = high, low
        es[k] = product(thi[...], tlo[...], high, low, ((1,), (0,)))

        @pl.when(z == 0)
        def _():
            for line in range(last, 0, -1):
                there = ru.at[k, block(line)]
                send(es.at[k, block(line)], there, ru_s.at[line], ru_r.at[line, k], up)

        @pl.when(z == last)
        def _():
            for line in range(last):
                there = rd.at[k, block(line)]
                send(es.at[k, block(line)], there, rd_s.at[line], rd_r.at[line, k], down)

    def add_on(k):
        for line in range(last, 1, -1):
            at = block(line)

            @pl.when((z > 0) & (z < line))
            def _():
                arrived(ru.at[k, at], ru_r.at[line, k])
                es[k, at, :] += ru[k, at, :]
                send(es.at[k, at], ru.at[k, at], ru_s.at[line], ru_r.at[line, k], up)

        for line in range(last - 1):
            at = block(line)

            @pl.when((z < last) & (z > line))
            def _():
                arrived(rd.at[k, at], rd_r.at[line, k])
                es[k, at, :] += rd[k, at, :]
                send(es.at[k, at], rd.at[k, at], rd_s.at[line], rd_r.at[line, k], down)

    def finish_expr(k):
        at = block(z)
        ge[:, cols(k)] = es[k, at, :]

        @pl.when(z > 0)
        def _():
            arrived(ru.at[k, at], ru_r.at[z, k])
            ge[:, cols(k)] += ru[k, at, :]

        @pl.when(z < last)
        def _():
            arrived(rd.at[k, at], rd_r.at[z, k])
            ge[:, cols(k)] += rd[k, at, :]

    def probs_gradient(at):
        return product(dhi[:, at], dlo[:, at], bhi[:, at], blo[:, at], ((1,), (1,)))

    added = 0
    middle = chunks // 2
    for k in range(chunks):
        backward_product(k)
        if k + AHEAD < chunks:
            send_grad(k + AHEAD)
        if k == middle - 1:
            fs[...] = probs_gradient(pl.ds(0, middle * width))
        while 3 * (added + 1) <= 2 * k:
            add_on(added)
            added += 1
    fs[...] += probs_gradient(pl.ds(middle * width, genes - middle * width))
    inner = jnp.sum(sacc[0], axis=1, keepdims=True)
    inn[core] = jnp.where(wide == 0, inner, gene_sum)
    send(inn.at[core], inn.at[core], in_s, in_r, sibling)

    for p in mates:
        send(fs.at[share(p)], fr.at[q], f_s, f_r.at[q], mate(p))
    fr[q] = fs[share(q), :]
    send(fr.at[q], fo.at[q], fo_s, fo_r.at[q], sibling)
    for p in mates:
        arrived(l1.at[p], l1_r.at[p])
    l2[z] = (l1[0] + l1[1]) + (l1[2] + l1[3])
    for o in others:
        send(l2.at[z], l2.at[z], l2_s, l2_r.at[z], (o * PLANE + q, core))
    while added < chunks - 1:
        add_on(added)
        added += 1
    for p in (mates[1], mates[2], mates[0]):
        arrived(fr.at[p], f_r.at[p])
        send(fr.at[p], fo.at[p], fo_s, fo_r.at[p], sibling)
    add_on(chunks - 1)
    for k in range(chunks - 2):
        finish_expr(k)

    arrived(inn.at[1 - core], in_r)
    both = inn[0] + inn[1]
    rowv[1] = jnp.broadcast_to(dmass, (rows, LANES))
    rowv[2] = jnp.broadcast_to(both[:, 0:1] + dmass * mass, (rows, LANES))
    for p in range(PLANE):
        arrived(fo.at[p], fo_r.at[p])

    @pl.loop(0, rows // STEP_ROWS)
    def _(step):
        at = pl.ds(pl.multiple_of(step * STEP_ROWS, STEP_ROWS), STEP_ROWS)
        by_mass, total_inner = rowv[1, at, 0:1], rowv[2, at, 0:1]
        for p in range(PLANE):
            for line in range(lines):
                here, there = pl.ds(line * cb, cb), (line * PLANE + p) * cb
                grad = fr[p, at, here] + fo[p, at, here] + by_mass * weights[:, there : there + cb]
                go[at, pl.ds(there, cb)] = pq[p, at, here] * (grad - total_inner)

    for m in range(slides):
        pltpu.make_async_copy(go.at[half(m)], glog_ref.at[m], out_s.at[slides + 1 + m]).start()

    for o in others:
        arrived(l2.at[o], l2_r.at[o])
    loss = l2[0]
    for line in range(1, lines):
        loss = loss + l2[line]
    loss_ref[...] = loss[0:1, 0:1] - both[0:1, 1:2]
    finish_expr(chunks - 2)
    finish_expr(chunks - 1)
    pltpu.make_async_copy(ge, gexp_ref, out_s.at[slides]).start()

    for m in range(slides):
        pltpu.make_async_copy(pr.at[half(m)], pred_ref.at[m], out_s.at[m]).wait()
        pltpu.make_async_copy(go.at[half(m)], glog_ref.at[m], out_s.at[slides + 1 + m]).wait()
    pltpu.make_async_copy(ge, gexp_ref, out_s.at[slides]).wait()
    for line in range(lines):
        at = block(line)

        @pl.when((line <= z) & (z < last))
        def _():
            sent(bb.at[:, at], ag_us.at[line])

        @pl.when((line >= z) & (z > 0))
        def _():
            sent(bb.at[:, at], ag_ds.at[line])

        @pl.when(line > z)
        def _():
            sent(es.at[:, at], ru_s.at[line])

        @pl.when(line < z)
        def _():
            sent(es.at[:, at], rd_s.at[line])

    three = pl.ds(0, len(mates))
    sent(ab.at[three, half(0)], a_s)
    sent(ab.at[three, half(0)], a2_s)
    sent(rs.at[three], r_s)
    sent(cr.at[:, three], c_s)
    sent(s1.at[three], s1_s)
    sent(s2.at[pl.ds(0, last)], s2_s)
    sent(ss.at[0], ss_s)
    sent(cr.at[:, three], d_s)
    sent(inn.at[0], in_s)
    sent(l1.at[three], l1_s)
    sent(l2.at[pl.ds(0, last)], l2_s)
    sent(fr.at[three], f_s)
    sent(fo, fo_s)


def grouped(refs, sizes):
    at = 0
    for size in sizes:
        yield refs[at : at + size]
        at += size


def deliver(pred_in, glog_in, gexp_in, pred_ref, glog_ref, gexp_ref, pred_mid, glog_mid, gexp_mid, sems):
    triples = ((glog_in, glog_mid, glog_ref), (pred_in, pred_mid, pred_ref), (gexp_in, gexp_mid, gexp_ref))
    loads = [pltpu.make_async_copy(src, mid, sems.at[0, at]) for at, (src, mid, _) in enumerate(triples)]
    stores = [pltpu.make_async_copy(mid, dst, sems.at[1, at]) for at, (_, mid, dst) in enumerate(triples)]
    for load in loads:
        load.start()
    for load, store in zip(loads, stores):
        load.wait()
        store.start()
    for store in stores:
        store.wait()


def plane_call(logits, expr, spatial, slide_spots, spot_cells, cell_prior, lines, chunks):
    slides, slide_rows, cells = logits.shape
    rows = slides * slide_rows
    cb, genes = expr.shape
    quarter = lines * cb
    spots = PLANE * rows
    width = genes // chunks
    dma = pltpu.SemaphoreType.DMA
    vmem = pltpu.VMEM
    anywhere = pl.BlockSpec(memory_space=pl.ANY)
    in_vmem = pl.BlockSpec(memory_space=pltpu.VMEM)
    in_smem = pl.BlockSpec(memory_space=pltpu.SMEM)
    scratch = [
        vmem((rows, cells), F32),
        vmem((PLANE, slide_rows, quarter), F32),
        vmem((rows, genes), F32),
        vmem((cb, genes), F32),
        vmem((PLANE, rows, quarter), F32),
        vmem((PLANE, rows, quarter), F32),
        vmem((PLANE, rows, quarter), F32),
        vmem((spots, quarter), BF16),
        vmem((spots, quarter), BF16),
        vmem((quarter, spots), BF16),
        vmem((quarter, spots), BF16),
        vmem((chunks, quarter, width), F32),
        vmem((quarter, genes), BF16),
        vmem((quarter, genes), BF16),
        vmem((chunks, spots, width), F32),
        vmem((chunks, PLANE, rows, width), F32),
        vmem((rows, genes), F32),
        vmem((3, rows, width), F32),
        vmem((PLANE, 8, genes), F32),
        vmem((lines, 8, genes), F32),
        vmem((8, genes), F32),
        vmem((2, rows, LANES), F32),
        vmem((3, rows, LANES), F32),
        vmem((PLANE, 8, rows), F32),
        vmem((chunks, spots, width), F32),
        vmem((spots, genes), BF16),
        vmem((spots, genes), BF16),
        vmem((chunks, quarter, width), F32),
        vmem((chunks, quarter, width), F32),
        vmem((chunks, quarter, width), F32),
        vmem((spots, quarter), F32),
        vmem((PLANE, rows, quarter), F32),
        vmem((PLANE, rows, quarter), F32),
        vmem((rows, cells), F32),
        vmem((cb, genes), F32),
        vmem((2, rows, LANES), F32),
        vmem((PLANE, 8, LANES), F32),
        vmem((lines, 8, LANES), F32),
        dma((2 * slides + 1,)),
        dma((lines, chunks)),
        dma((lines,)),
        dma((lines,)),
        dma,
        dma((PLANE,)),
        dma,
        dma((PLANE,)),
        dma,
        dma((PLANE,)),
        dma,
        dma((chunks, PLANE)),
        dma,
        dma((2, PLANE)),
        dma,
        dma((2, lines)),
        dma,
        dma,
        dma,
        dma((chunks, PLANE)),
        dma((lines,)),
        dma((lines, chunks)),
        dma((lines,)),
        dma((lines, chunks)),
        dma,
        dma((PLANE,)),
        dma,
        dma((PLANE,)),
        dma,
        dma,
        dma,
        dma((PLANE,)),
        dma,
        dma((lines,)),
        dma((2 * slides + 1,)),
    ]
    pred_shape = jax.ShapeDtypeStruct((slides, slide_rows, genes), F32)
    glog_shape = jax.ShapeDtypeStruct((slides, slide_rows, cells), F32)
    gexp_shape = jax.ShapeDtypeStruct((cb, genes), F32)
    pred, loss, grad_logits, grad_expr = pl.pallas_call(
        functools.partial(plane_kernel, lines, chunks),
        out_shape=(pred_shape, jax.ShapeDtypeStruct((1, 1), F32), glog_shape, gexp_shape),
        in_specs=[anywhere, anywhere, anywhere, in_smem, in_vmem, in_vmem],
        out_specs=(anywhere, in_vmem, anywhere, anywhere),
        scratch_shapes=scratch,
        compiler_params=pltpu.CompilerParams(
            collective_id=0, has_side_effects=True, vmem_limit_bytes=56 * 1024 * 1024
        ),
    )(logits, expr, spatial, slide_spots, spot_cells, cell_prior.reshape(1, cells))
    pred, grad_logits, grad_expr = pl.pallas_call(
        deliver,
        out_shape=(pred_shape, glog_shape, gexp_shape),
        in_specs=[anywhere] * 3,
        out_specs=(anywhere,) * 3,
        scratch_shapes=[vmem(shape.shape, F32) for shape in (pred_shape, glog_shape, gexp_shape)] + [dma((2, 3))],
        compiler_params=pltpu.CompilerParams(vmem_limit_bytes=56 * 1024 * 1024),
    )(pred, grad_logits, grad_expr)
    return pred, loss.reshape(()), grad_logits, grad_expr


def general_plan(logits, expr, spatial, slide_spots, spot_cells, cell_prior):
    place = lax.axis_index("spot")
    side = lax.axis_index("gene")
    rows_all = logits.shape[1]
    cell_rows = expr.shape[0]
    weights = cell_prior.astype(jnp.float32) / fixed_point
    gene_share = (place == 0).astype(jnp.float32)
    row_share = (side == 0).astype(jnp.float32)
    own_weights = lax.dynamic_slice_in_dim(weights, place * cell_rows, cell_rows, 0)
    expr_acc = jnp.zeros((cell_rows, expr.shape[1]), jnp.float32)
    loss_local = jnp.zeros((), jnp.float32)
    pred_list = []
    grad_list = []
    for slide in range(logits.shape[0]):
        logit_rows = logits[slide]
        counted = spot_cells[slide].astype(jnp.float32)
        target = spatial[slide]
        positions = place * rows_all + jnp.arange(rows_all, dtype=jnp.int32)
        valid = (positions < slide_spots[slide]).astype(jnp.float32)
        peak = jnp.max(logit_rows, axis=1, keepdims=True)
        raised = jnp.exp(logit_rows - peak)
        probs = raised / jnp.sum(raised, axis=1, keepdims=True)
        mass = jnp.dot(probs, weights, precision=lax.Precision.HIGHEST)
        blocks = lax.all_to_all(probs, "spot", split_axis=1, concat_axis=0, tiled=True)
        pred = lax.psum_scatter(
            jnp.dot(blocks, expr, precision=lax.Precision.HIGHEST),
            "spot",
            scatter_dimension=0,
            tiled=True,
        )
        gene_dot = jnp.sum(valid[:, None] * pred * target, axis=0)
        gene_pred = jnp.sum(valid[:, None] * pred * pred, axis=0)
        gene_true = jnp.sum(valid[:, None] * target * target, axis=0)
        mass_part = jnp.sum(valid * mass)
        kcell = valid * counted
        cell_part = jnp.sum(kcell)
        spot_dot = jnp.sum(pred * target, axis=1)
        spot_pred = jnp.sum(pred * pred, axis=1)
        spot_true = jnp.sum(target * target, axis=1)
        gene_dot, gene_pred, gene_true, mass_total, cell_total = lax.psum(
            (gene_dot, gene_pred, gene_true, mass_part, cell_part), "spot"
        )
        spot_dot, spot_pred, spot_true = lax.psum((spot_dot, spot_pred, spot_true), "gene")
        gene_inv = lax.rsqrt(gene_pred * gene_true + tiny)
        cos_gene = gene_dot * gene_inv
        spot_inv = lax.rsqrt(spot_pred * spot_true + tiny)
        cos_spot = spot_dot * spot_inv
        share = kcell / cell_total
        scale_count = slide_spots[slide].astype(jnp.float32)
        kl_part = jnp.sum(
            share * (jnp.log(counted) - jnp.log(cell_total) - jnp.log(mass) + jnp.log(mass_total))
        )
        loss_local = loss_local - gene_share * jnp.sum(cos_gene)
        loss_local = loss_local + row_share * (scale_count * kl_part - jnp.sum(valid * cos_spot))
        gene_back = cos_gene * gene_true / (gene_pred * gene_true + tiny)
        spot_back = cos_spot * spot_true / (spot_pred * spot_true + tiny)
        dpred = -valid[:, None] * (
            target * (gene_inv[None, :] + spot_inv[:, None])
            - pred * gene_back[None, :]
            - pred * spot_back[:, None]
        )
        dmass = scale_count * valid * (1.0 / mass_total - share / mass)
        pred_list.append(pred)
        grads_full, mass_full = (
            lax.all_gather(dpred, "spot", axis=0, tiled=True),
            lax.all_gather(dmass, "spot", axis=0, tiled=True),
        )
        dprob_cells = jnp.dot(grads_full, expr.T, precision=lax.Precision.HIGHEST)
        dprob_cells = lax.psum(dprob_cells, "gene")
        expr_acc = expr_acc + lax.dot_general(
            blocks, grads_full, (((0,), (0,)), ((), ())), precision=lax.Precision.HIGHEST
        )
        dprob_cells = dprob_cells + mass_full[:, None] * own_weights[None, :]
        dprob_rows = lax.all_to_all(dprob_cells, "spot", split_axis=0, concat_axis=1, tiled=True)
        inner = jnp.sum(probs * dprob_rows, axis=1, keepdims=True)
        dlogit = probs * (dprob_rows - inner)
        grad_list.append(dlogit)
    loss = lax.psum(loss_local, ("spot", "gene"))
    return (jnp.stack(pred_list), loss, jnp.stack(grad_list), expr_acc)


def solution(mesh):
    places = mesh.shape["spot"]

    def on_device(logits, expr, spatial, slide_spots, spot_cells, cell_prior):
        if places == PLANE * PLANE and mesh.shape["gene"] == 2 and logits.shape[2] * expr.shape[1] <= 1 << 21:
            return plane_call(
                logits, expr, spatial, slide_spots, spot_cells, cell_prior, places // PLANE, CHUNKS
            )
        return general_plan(logits, expr, spatial, slide_spots, spot_cells, cell_prior)

    in_specs = (
        P(None, "spot", None),
        P("spot", "gene"),
        P(None, "spot", "gene"),
        P(),
        P(None, "spot"),
        P(),
    )
    out_specs = (P(None, "spot", "gene"), P(), P(None, "spot", None), P("spot", "gene"))
    return jax.shard_map(
        on_device, mesh=mesh, in_specs=in_specs, out_specs=out_specs, check_vma=False
    )
```

```python
import functools

import jax
import jax.numpy as jnp
from jax import lax
from jax.experimental import pallas as pl
from jax.experimental.pallas import tpu as pltpu
from jax.sharding import PartitionSpec as P

tiny = 1e-06
fixed_point = 16384.0
F32 = jnp.float32
BF16 = jnp.bfloat16
MESH = pl.DeviceIdType.MESH

PLANE = 4
LANES = 128
STEP_ROWS = 16
FORWARD = (256, 256, 256, 256)
BACKWARD = (256, 256, 256, 256)
LEAD = 2
LAG = 1
AHEAD = 2


def halves(value):
    high = value.astype(BF16)
    return high, (value - high.astype(F32)).astype(BF16)


def product(a_high, a_low, b_high, b_low, contract):
    def one(a, b):
        return lax.dot_general(a, b, (contract, ((), ())), preferred_element_type=F32)

    return one(a_high, b_high) + (one(a_high, b_low) + one(a_low, b_high))


def plane_kernel(lines, forward_widths, backward_widths, *refs):
    chunks, turns = len(forward_widths), len(backward_widths)
    (
        (logits_ref, expr_ref, spatial_ref, count_ref, cells_ref, prior_ref),
        (pred_ref, loss_ref, glog_ref, gexp_ref),
        (lg, lq, tg, ex, pq, ab, af, ahi, alo, thi, tlo, bhi, blo, pr, sacc, s1, s2, gv, ss, rowv, rs),
        (dhi, dlo, fs, fr, fo, go, ge, inn, l1, l2),
        (loc, ou_s, ou_r, od_s, od_r, fu_s, fu_r, fd_s, fd_r, a_s, a_r, a2_s, a2_r, r_s, r_r),
        (c_s, c_r, s1_s, s1_r, s2_s, s2_r, ss_s, ss_r, d_s, d_r, ru_s, ru_r, rd_s, rd_r),
        (f_s, f_r, fo_s, fo_r, in_s, in_r, l1_s, l1_r, l2_s, l2_r, out_s),
        bb,
        cs,
        cr,
        ds,
        es,
        ru,
        rd,
    ) = grouped(refs, (6, 4, 21, 10, 15, 14, 11, chunks, chunks, chunks, turns, turns, turns, turns))
    place = lax.axis_index("spot")
    core = lax.axis_index("gene")
    z = place // PLANE
    q = place % PLANE
    col, row = q % 2, q // 2
    mates = ((1 - row) * 2 + 1 - col, row * 2 + 1 - col, (1 - row) * 2 + col)
    others = tuple((z + step) % lines for step in range(1, lines))
    up, down = (place + PLANE, core), (place - PLANE, core)
    sibling = (place, 1 - core)
    slides, slide_rows = logits_ref.shape[0], logits_ref.shape[1]
    rows = slides * slide_rows
    cb = expr_ref.shape[0]
    genes = expr_ref.shape[1]
    last = lines - 1
    at_end = (z == 0) | (z == last)
    in_middle = (z > 0) & (z < last)

    def mate(p):
        return (z * PLANE + p, core)

    def send(src, dst, send_sem, recv_sem, device):
        copy = pltpu.make_async_remote_copy(
            src_ref=src, dst_ref=dst, send_sem=send_sem, recv_sem=recv_sem, device_id=device, device_id_type=MESH
        )
        copy.start()

    def arrived(dst, recv_sem):
        pltpu.make_async_copy(dst, dst, recv_sem).wait()

    sent = arrived

    def cols(k):
        return pl.ds(sum(forward_widths[:k]), forward_widths[k])

    def turn_cols(k):
        return pl.ds(sum(backward_widths[:k]), backward_widths[k])

    def block(index):
        return pl.ds(pl.multiple_of(index * cb, cb), cb)

    def share(index):
        return pl.ds(pl.multiple_of(index * rows, rows), rows)

    def half(index):
        return pl.ds(pl.multiple_of(index * slide_rows, slide_rows), slide_rows)

    for m in range(slides):
        pltpu.make_async_copy(logits_ref.at[m], lg.at[half(m)], loc.at[m]).start()
        pltpu.make_async_copy(spatial_ref.at[m], tg.at[half(m)], loc.at[slides + m]).start()
    pltpu.make_async_copy(expr_ref, ex, loc.at[2 * slides]).start()

    barrier = pltpu.get_barrier_semaphore()
    for p in mates:
        pl.semaphore_signal(barrier, inc=1, device_id=mate(p), device_id_type=MESH)
    for o in others:
        pl.semaphore_signal(barrier, inc=1, device_id=(o * PLANE + q, core), device_id_type=MESH)
    pl.semaphore_signal(barrier, inc=1, device_id=sibling, device_id_type=MESH)
    pl.semaphore_wait(barrier, len(mates) + len(others) + 1)

    for m in range(slides):
        pltpu.make_async_copy(logits_ref.at[m], lg.at[half(m)], loc.at[m]).wait()
    for p in range(PLANE):
        for line in range(lines):
            lq[p, :, pl.ds(line * cb, cb)] = lg[half(core), pl.ds((line * PLANE + p) * cb, cb)]
    for p in mates:
        send(lq.at[p], ab.at[q, half(core)], a_s, a_r.at[q], mate(p))

    pltpu.make_async_copy(expr_ref, ex, loc.at[2 * slides]).wait()
    for k in range(chunks):
        bb[k][block(z), :] = ex[:, cols(k)]

    def send_own(k):
        here = bb[k].at[block(z)]

        @pl.when(z < last)
        def _():
            send(here, here, ou_s.at[k], ou_r.at[k], up)

        @pl.when(z > 0)
        def _():
            send(here, here, od_s.at[k], od_r.at[k], down)

    for k in range(min(LEAD, chunks)):
        send_own(k)

    @pl.when(at_end)
    def _():
        for k in range(LEAD, chunks):
            send_own(k)

    def from_below(k, at):
        arrived(bb[k].at[pl.ds((at - 1) * cb, cb)], ou_r.at[k])
        if at > 1:
            arrived(bb[k].at[pl.ds(0, (at - 1) * cb)], fu_r.at[k])

    def from_above(k, at):
        arrived(bb[k].at[pl.ds((at + 1) * cb, cb)], od_r.at[k])
        if at < last - 1:
            arrived(bb[k].at[pl.ds((at + 2) * cb, (last - 1 - at) * cb)], fd_r.at[k])

    def forward(k):
        for at in range(1, last):

            @pl.when(z == at)
            def _():
                def upward():
                    from_below(k, at)
                    here = bb[k].at[pl.ds(0, at * cb)]
                    send(here, here, fu_s.at[k], fu_r.at[k], up)

                def downward():
                    from_above(k, at)
                    here = bb[k].at[pl.ds((at + 1) * cb, (last - at) * cb)]
                    send(here, here, fd_s.at[k], fd_r.at[k], down)

                for step in (upward, downward) if 2 * at < lines else (downward, upward):
                    step()
                if k + LEAD < chunks:
                    send_own(k + LEAD)

    def gathered(k):
        @pl.when(z == 0)
        def _():
            from_above(k, 0)

        @pl.when(z == last)
        def _():
            from_below(k, last)

    weights = prior_ref[...].astype(F32) / fixed_point

    @pl.loop(0, rows // STEP_ROWS)
    def _(step):
        at = pl.ds(pl.multiple_of(step * STEP_ROWS, STEP_ROWS), STEP_ROWS)
        value = lg[at, :]
        peak = jnp.max(value, axis=1, keepdims=True)
        raised = jnp.exp(value - peak)
        scale = 1.0 / jnp.sum(raised, axis=1, keepdims=True)
        probs = raised * scale
        mass_rows = jnp.sum(probs * weights, axis=1, keepdims=True)
        rowv[0, at, :] = jnp.broadcast_to(mass_rows, (STEP_ROWS, LANES))
        rowv[1, at, :] = jnp.broadcast_to(peak, (STEP_ROWS, LANES))
        rowv[2, at, :] = jnp.broadcast_to(scale, (STEP_ROWS, LANES))
        for p in range(PLANE):
            for line in range(lines):
                at_cells = (line * PLANE + p) * cb
                pq[p, at, pl.ds(line * cb, cb)] = probs[:, at_cells : at_cells + cb]

    wide = lax.broadcasted_iota(jnp.int32, (rows, LANES), 1)
    rs[q] = jnp.where(wide == 0, rowv[1], rowv[2]).T[0:8]
    for p in mates:
        send(rs.at[q], rs.at[q], r_s, r_r.at[q], mate(p))

    for p in (mates[1], mates[2], mates[0]):
        here = ab.at[p, half(core)]
        arrived(here, a_r.at[p])
        send(here, here, a2_s, a2_r.at[p], sibling)
    forward(0)

    rid = lax.broadcasted_iota(jnp.int32, (rows, 1), 0)
    first = rid < slide_rows
    position = place * slide_rows + jnp.where(first, rid, rid - slide_rows)
    count = jnp.where(first, count_ref[0], count_ref[1])
    valid = (position < count).astype(F32)
    scale_count = count.astype(F32)
    square = (slide_rows, slide_rows)
    eye = lax.broadcasted_iota(jnp.int32, square, 0) == lax.broadcasted_iota(jnp.int32, square, 1)
    counted = jnp.concatenate(
        [
            jnp.sum(jnp.where(eye, cells_ref[m : m + 1, :].astype(F32), 0.0), axis=1, keepdims=True)
            for m in range(slides)
        ],
        axis=0,
    )
    mass = rowv[0, :, 0:1]
    kcell = valid * counted

    def by_slide(value):
        return [jnp.sum(value[m * slide_rows : (m + 1) * slide_rows], axis=0, keepdims=True) for m in range(slides)]

    mass_parts = by_slide(valid * mass)
    cell_parts = by_slide(kcell)
    lane = lax.broadcasted_iota(jnp.int32, (1, LANES), 1)
    scalars = jnp.zeros((1, LANES), F32)
    for at, value in enumerate(mass_parts + cell_parts):
        scalars = jnp.where(lane == at, value, scalars)
    for m in range(slides):
        pltpu.make_async_copy(spatial_ref.at[m], tg.at[half(m)], loc.at[slides + m]).wait()
    sacc[...] = jnp.zeros_like(sacc)
    s1[q, 3 * slides :, :] = jnp.zeros((8 - 3 * slides, genes), F32)
    s1[q, 3 * slides : 3 * slides + 1, 0:LANES] = scalars

    af[q] = pq[q]
    ahi[share(q), :], alo[share(q), :] = halves(pq[q])
    for p in (mates[1], mates[2], mates[0]):
        arrived(rs.at[p], r_r.at[p])
        arrived(ab.at[p, half(1 - core)], a2_r.at[p])
        by_row = rs[p].T
        probs = jnp.exp(ab[p] - by_row[:, 0:1]) * by_row[:, 1:2]
        af[p] = probs
        ahi[share(p), :], alo[share(p), :] = halves(probs)

    def forward_product(k):
        gathered(k)
        high, low = halves(bb[k][...])
        bhi[:, cols(k)], blo[:, cols(k)] = high, low
        cs[k][...] = product(ahi[...], alo[...], high, low, ((1,), (0,)))
        for p in mates:
            send(cs[k].at[share(p)], cr[k].at[q], c_s.at[k], c_r.at[k, q], mate(p))

    def finish_pred(k):
        total = cs[k][share(q), :]
        for p in mates:
            arrived(cr[k].at[p], c_r.at[k, p])
            total = total + cr[k][p]
        pr[:, cols(k)] = total
        truth = tg[:, cols(k)]
        for at, value in enumerate((total * truth, total * total, truth * truth)):
            sacc[at] += lane_groups(value)
        kept = valid * total
        stats = by_slide(kept * truth) + by_slide(kept * total) + by_slide(valid * truth * truth)
        s1[q, 0 : 3 * slides, cols(k)] = jnp.concatenate(stats, axis=0)

    early = sum(forward_widths[: chunks - LAG])
    parts = (pl.ds(0, early), pl.ds(early, genes - early))

    def sum_plane(at):
        for p in mates:
            send(s1.at[q, :, parts[at]], s1.at[q, :, parts[at]], s1_s, s1_r.at[at, q], mate(p))

    def sum_line(at):
        for p in mates:
            arrived(s1.at[p, :, parts[at]], s1_r.at[at, p])
        s2[z, :, parts[at]] = (s1[0, :, parts[at]] + s1[1, :, parts[at]]) + (s1[2, :, parts[at]] + s1[3, :, parts[at]])
        for o in others:
            send(s2.at[z, :, parts[at]], s2.at[z, :, parts[at]], s2_s, s2_r.at[at, z], (o * PLANE + q, core))

    for k in range(chunks):
        if k + 1 < chunks:
            forward(k + 1)
        forward_product(k)
        if k >= LAG:
            finish_pred(k - LAG)
    sum_plane(0)
    for p in range(PLANE):
        high, low = halves(af[p].T)
        thi[:, share(p)], tlo[:, share(p)] = high, low
    sum_line(0)
    for k in range(chunks - LAG, chunks):
        finish_pred(k)
    sum_plane(1)
    for m in range(slides):
        pltpu.make_async_copy(pr.at[half(m)], pred_ref.at[m], out_s.at[m]).start()

    sums = [jnp.sum(sacc[at], axis=1, keepdims=True) for at in range(3)]
    ss[core] = jnp.where(wide == 0, sums[0], jnp.where(wide == 1, sums[1], sums[2]))
    send(ss.at[core], ss.at[core], ss_s, ss_r, sibling)
    sum_line(1)
    arrived(ss.at[1 - core], ss_r)
    spot = ss[0] + ss[1]
    spot_dot, spot_pred, spot_true = spot[:, 0:1], spot[:, 1:2], spot[:, 2:3]
    spot_inv = lax.rsqrt(spot_pred * spot_true + tiny)
    cos_spot = spot_dot * spot_inv
    spot_back = cos_spot * spot_true / (spot_pred * spot_true + tiny)
    for o in others:
        for at in range(2):
            arrived(s2.at[o, :, parts[at]], s2_r.at[at, o])
    total = s2[0]
    for line in range(1, lines):
        total = total + s2[line]
    gene_dot, gene_pred, gene_true = total[0:2], total[2:4], total[4:6]
    gene_inv = lax.rsqrt(gene_pred * gene_true + tiny)
    cos_gene = gene_dot * gene_inv
    gv[0:2, :] = gene_inv
    gv[2:4, :] = cos_gene * gene_true / (gene_pred * gene_true + tiny)

    sacc[0] = jnp.zeros_like(sacc[0])

    def send_grad(k):
        pieces = []
        for m in range(slides):
            lo, hi = m * slide_rows, (m + 1) * slide_rows
            truth, guess = tg[lo:hi, turn_cols(k)], pr[lo:hi, turn_cols(k)]
            inverse, back = gv[m : m + 1, turn_cols(k)], gv[2 + m : 3 + m, turn_cols(k)]
            pieces.append(
                -valid[lo:hi]
                * (truth * (inverse + spot_inv[lo:hi]) - guess * back - guess * spot_back[lo:hi])
            )
        grad = jnp.concatenate(pieces, axis=0)
        here = ds[k].at[share(q)]
        here[...] = grad
        for p in mates:
            send(here, here, d_s.at[k], d_r.at[k, q], mate(p))
        sacc[0] += lane_groups(grad * pr[:, turn_cols(k)])

    for k in range(min(AHEAD, turns)):
        send_grad(k)
    gene_sum = jnp.sum(jnp.sum(cos_gene, axis=1, keepdims=True), axis=0, keepdims=True)

    mass_total = jnp.where(first, total[6:7, 0:1], total[6:7, 1:2])
    cell_total = jnp.where(first, total[6:7, 2:3], total[6:7, 3:4])
    portion = kcell / cell_total
    kl_rows = portion * (jnp.log(counted) - jnp.log(cell_total) - jnp.log(mass) + jnp.log(mass_total))
    dmass = scale_count * valid * (1.0 / mass_total - portion / mass)
    terms = jnp.sum(scale_count * kl_rows - valid * cos_spot, axis=0, keepdims=True)
    l1[q] = jnp.broadcast_to(terms, (8, LANES))
    for p in mates:
        send(l1.at[q], l1.at[q], l1_s, l1_r.at[q], mate(p))

    def backward_product(k):
        for p in mates:
            arrived(ds[k].at[share(p)], d_r.at[k, p])
        high, low = halves(ds[k][...])
        dhi[:, turn_cols(k)], dlo[:, turn_cols(k)] = high, low
        es[k][...] = product(thi[...], tlo[...], high, low, ((1,), (0,)))

        @pl.when(z == 0)
        def _():
            above = pl.ds(cb, last * cb)
            send(es[k].at[above], ru[k].at[above], ru_s.at[k], ru_r.at[k], up)

        @pl.when(z == last)
        def _():
            below = pl.ds(0, last * cb)
            send(es[k].at[below], rd[k].at[below], rd_s.at[k], rd_r.at[k], down)

    def add_on(k):
        for at in range(1, last):

            @pl.when(z == at)
            def _():
                def upward():
                    arrived(ru[k].at[pl.ds(at * cb, (lines - at) * cb)], ru_r.at[k])
                    above = pl.ds((at + 1) * cb, (last - at) * cb)
                    es[k][above, :] += ru[k][above, :]
                    send(es[k].at[above], ru[k].at[above], ru_s.at[k], ru_r.at[k], up)

                def downward():
                    arrived(rd[k].at[pl.ds(0, (at + 1) * cb)], rd_r.at[k])
                    below = pl.ds(0, at * cb)
                    es[k][below, :] += rd[k][below, :]
                    send(es[k].at[below], rd[k].at[below], rd_s.at[k], rd_r.at[k], down)

                for step in (upward, downward) if 2 * at < lines else (downward, upward):
                    step()

    def finish_expr(k):
        own = block(z)

        @pl.when(z == 0)
        def _():
            arrived(rd[k].at[own], rd_r.at[k])
            ge[:, turn_cols(k)] = es[k][own, :] + rd[k][own, :]

        @pl.when(z == last)
        def _():
            arrived(ru[k].at[own], ru_r.at[k])
            ge[:, turn_cols(k)] = es[k][own, :] + ru[k][own, :]

        @pl.when(in_middle)
        def _():
            ge[:, turn_cols(k)] = es[k][own, :] + (ru[k][own, :] + rd[k][own, :])

    def probs_gradient(at):
        return product(dhi[:, at], dlo[:, at], bhi[:, at], blo[:, at], ((1,), (1,)))

    added = 0
    middle = turns // 2
    fold = sum(backward_widths[:middle])
    for k in range(turns):
        backward_product(k)
        if k + AHEAD < turns:
            send_grad(k + AHEAD)
        if k == middle - 1:
            fs[...] = probs_gradient(pl.ds(0, fold))
        while 3 * (added + 1) <= 2 * k:
            add_on(added)
            added += 1
    fs[...] += probs_gradient(pl.ds(fold, genes - fold))
    inner = jnp.sum(sacc[0], axis=1, keepdims=True)
    inn[core] = jnp.where(wide == 0, inner, gene_sum)
    send(inn.at[core], inn.at[core], in_s, in_r, sibling)

    for p in mates:
        send(fs.at[share(p)], fr.at[q], f_s, f_r.at[q], mate(p))
    fr[q] = fs[share(q), :]
    send(fr.at[q], fo.at[q], fo_s, fo_r.at[q], sibling)
    for p in mates:
        arrived(l1.at[p], l1_r.at[p])
    l2[z] = (l1[0] + l1[1]) + (l1[2] + l1[3])
    for o in others:
        send(l2.at[z], l2.at[z], l2_s, l2_r.at[z], (o * PLANE + q, core))
    while added < turns - 1:
        add_on(added)
        added += 1
    for p in (mates[1], mates[2], mates[0]):
        arrived(fr.at[p], f_r.at[p])
        send(fr.at[p], fo.at[p], fo_s, fo_r.at[p], sibling)
    add_on(turns - 1)
    for k in range(turns - 2):
        finish_expr(k)

    arrived(inn.at[1 - core], in_r)
    both = inn[0] + inn[1]
    rowv[1] = jnp.broadcast_to(dmass, (rows, LANES))
    rowv[2] = jnp.broadcast_to(both[:, 0:1] + dmass * mass, (rows, LANES))
    for p in range(PLANE):
        arrived(fo.at[p], fo_r.at[p])

    @pl.loop(0, rows // STEP_ROWS)
    def _(step):
        at = pl.ds(pl.multiple_of(step * STEP_ROWS, STEP_ROWS), STEP_ROWS)
        by_mass, total_inner = rowv[1, at, 0:1], rowv[2, at, 0:1]
        for p in range(PLANE):
            for line in range(lines):
                here, there = pl.ds(line * cb, cb), (line * PLANE + p) * cb
                grad = fr[p, at, here] + fo[p, at, here] + by_mass * weights[:, there : there + cb]
                go[at, pl.ds(there, cb)] = pq[p, at, here] * (grad - total_inner)

    for m in range(slides):
        pltpu.make_async_copy(go.at[half(m)], glog_ref.at[m], out_s.at[slides + 1 + m]).start()

    for o in others:
        arrived(l2.at[o], l2_r.at[o])
    loss = l2[0]
    for line in range(1, lines):
        loss = loss + l2[line]
    loss_ref[...] = loss[0:1, 0:1] - both[0:1, 1:2]
    finish_expr(turns - 2)
    finish_expr(turns - 1)
    pltpu.make_async_copy(ge, gexp_ref, out_s.at[slides]).start()

    for m in range(slides):
        pltpu.make_async_copy(pr.at[half(m)], pred_ref.at[m], out_s.at[m]).wait()
        pltpu.make_async_copy(go.at[half(m)], glog_ref.at[m], out_s.at[slides + 1 + m]).wait()
    pltpu.make_async_copy(ge, gexp_ref, out_s.at[slides]).wait()
    for k in range(chunks):

        @pl.when(z < last)
        def _():
            sent(bb[k].at[block(z)], ou_s.at[k])

        @pl.when(z > 0)
        def _():
            sent(bb[k].at[block(z)], od_s.at[k])

        for at in range(1, last):

            @pl.when(z == at)
            def _():
                sent(bb[k].at[pl.ds(0, at * cb)], fu_s.at[k])
                sent(bb[k].at[pl.ds((at + 1) * cb, (last - at) * cb)], fd_s.at[k])

    for k in range(turns):
        for at in range(lines):

            @pl.when(z == at)
            def _():
                if at < last:
                    sent(es[k].at[pl.ds((at + 1) * cb, (last - at) * cb)], ru_s.at[k])
                if at > 0:
                    sent(es[k].at[pl.ds(0, at * cb)], rd_s.at[k])

    three = pl.ds(0, len(mates))
    sent(ab.at[three, half(0)], a_s)
    sent(ab.at[three, half(0)], a2_s)
    sent(rs.at[three], r_s)
    for k in range(chunks):
        sent(cr[k].at[three], c_s.at[k])
    sent(s1.at[three], s1_s)
    sent(s2.at[pl.ds(0, last)], s2_s)
    sent(ss.at[0], ss_s)
    for k in range(turns):
        sent(ds[k].at[pl.ds(0, len(mates) * rows)], d_s.at[k])
    sent(inn.at[0], in_s)
    sent(l1.at[three], l1_s)
    sent(l2.at[pl.ds(0, last)], l2_s)
    sent(fr.at[three], f_s)
    sent(fo, fo_s)


def lane_groups(value):
    parts = [value[:, at : at + LANES] for at in range(0, value.shape[1], LANES)]
    return functools.reduce(lambda a, b: a + b, parts)


def grouped(refs, sizes):
    at = 0
    for size in sizes:
        yield refs[at : at + size]
        at += size


def deliver(pred_in, glog_in, gexp_in, pred_ref, glog_ref, gexp_ref, pred_mid, glog_mid, gexp_mid, sems):
    triples = ((glog_in, glog_mid, glog_ref), (pred_in, pred_mid, pred_ref), (gexp_in, gexp_mid, gexp_ref))
    loads = [pltpu.make_async_copy(src, mid, sems.at[0, at]) for at, (src, mid, _) in enumerate(triples)]
    stores = [pltpu.make_async_copy(mid, dst, sems.at[1, at]) for at, (_, mid, dst) in enumerate(triples)]
    for load in loads:
        load.start()
    for load, store in zip(loads, stores):
        load.wait()
        store.start()
    for store in stores:
        store.wait()


def plane_call(logits, expr, spatial, slide_spots, spot_cells, cell_prior, lines):
    slides, slide_rows, cells = logits.shape
    rows = slides * slide_rows
    cb, genes = expr.shape
    quarter = lines * cb
    spots = PLANE * rows
    chunks, turns = len(FORWARD), len(BACKWARD)
    dma = pltpu.SemaphoreType.DMA
    vmem = pltpu.VMEM
    anywhere = pl.BlockSpec(memory_space=pl.ANY)
    in_vmem = pl.BlockSpec(memory_space=pltpu.VMEM)
    in_smem = pl.BlockSpec(memory_space=pltpu.SMEM)
    scratch = [
        vmem((rows, cells), F32),
        vmem((PLANE, slide_rows, quarter), F32),
        vmem((rows, genes), F32),
        vmem((cb, genes), F32),
        vmem((PLANE, rows, quarter), F32),
        vmem((PLANE, rows, quarter), F32),
        vmem((PLANE, rows, quarter), F32),
        vmem((spots, quarter), BF16),
        vmem((spots, quarter), BF16),
        vmem((quarter, spots), BF16),
        vmem((quarter, spots), BF16),
        vmem((quarter, genes), BF16),
        vmem((quarter, genes), BF16),
        vmem((rows, genes), F32),
        vmem((3, rows, LANES), F32),
        vmem((PLANE, 8, genes), F32),
        vmem((lines, 8, genes), F32),
        vmem((8, genes), F32),
        vmem((2, rows, LANES), F32),
        vmem((3, rows, LANES), F32),
        vmem((PLANE, 8, rows), F32),
        vmem((spots, genes), BF16),
        vmem((spots, genes), BF16),
        vmem((spots, quarter), F32),
        vmem((PLANE, rows, quarter), F32),
        vmem((PLANE, rows, quarter), F32),
        vmem((rows, cells), F32),
        vmem((cb, genes), F32),
        vmem((2, rows, LANES), F32),
        vmem((PLANE, 8, LANES), F32),
        vmem((lines, 8, LANES), F32),
        dma((2 * slides + 1,)),
        dma((chunks,)),
        dma((chunks,)),
        dma((chunks,)),
        dma((chunks,)),
        dma((chunks,)),
        dma((chunks,)),
        dma((chunks,)),
        dma((chunks,)),
        dma,
        dma((PLANE,)),
        dma,
        dma((PLANE,)),
        dma,
        dma((PLANE,)),
        dma((chunks,)),
        dma((chunks, PLANE)),
        dma,
        dma((2, PLANE)),
        dma,
        dma((2, lines)),
        dma,
        dma,
        dma((turns,)),
        dma((turns, PLANE)),
        dma((turns,)),
        dma((turns,)),
        dma((turns,)),
        dma((turns,)),
        dma,
        dma((PLANE,)),
        dma,
        dma((PLANE,)),
        dma,
        dma,
        dma,
        dma((PLANE,)),
        dma,
        dma((lines,)),
        dma((2 * slides + 1,)),
    ]
    for shape, widths in (
        ((quarter,), FORWARD),
        ((spots,), FORWARD),
        ((PLANE, rows), FORWARD),
        ((spots,), BACKWARD),
        ((quarter,), BACKWARD),
        ((quarter,), BACKWARD),
        ((quarter,), BACKWARD),
    ):
        scratch += [vmem(shape + (width,), F32) for width in widths]
    pred_shape = jax.ShapeDtypeStruct((slides, slide_rows, genes), F32)
    glog_shape = jax.ShapeDtypeStruct((slides, slide_rows, cells), F32)
    gexp_shape = jax.ShapeDtypeStruct((cb, genes), F32)
    pred, loss, grad_logits, grad_expr = pl.pallas_call(
        functools.partial(plane_kernel, lines, FORWARD, BACKWARD),
        out_shape=(pred_shape, jax.ShapeDtypeStruct((1, 1), F32), glog_shape, gexp_shape),
        in_specs=[anywhere, anywhere, anywhere, in_smem, in_vmem, in_vmem],
        out_specs=(anywhere, in_vmem, anywhere, anywhere),
        scratch_shapes=scratch,
        compiler_params=pltpu.CompilerParams(
            collective_id=0, has_side_effects=True, vmem_limit_bytes=56 * 1024 * 1024
        ),
    )(logits, expr, spatial, slide_spots, spot_cells, cell_prior.reshape(1, cells))
    pred, grad_logits, grad_expr = pl.pallas_call(
        deliver,
        out_shape=(pred_shape, glog_shape, gexp_shape),
        in_specs=[anywhere] * 3,
        out_specs=(anywhere,) * 3,
        scratch_shapes=[vmem(shape.shape, F32) for shape in (pred_shape, glog_shape, gexp_shape)] + [dma((2, 3))],
        compiler_params=pltpu.CompilerParams(vmem_limit_bytes=56 * 1024 * 1024),
    )(pred, grad_logits, grad_expr)
    return pred, loss.reshape(()), grad_logits, grad_expr


def general_plan(logits, expr, spatial, slide_spots, spot_cells, cell_prior):
    place = lax.axis_index("spot")
    side = lax.axis_index("gene")
    rows_all = logits.shape[1]
    cell_rows = expr.shape[0]
    weights = cell_prior.astype(jnp.float32) / fixed_point
    gene_share = (place == 0).astype(jnp.float32)
    row_share = (side == 0).astype(jnp.float32)
    own_weights = lax.dynamic_slice_in_dim(weights, place * cell_rows, cell_rows, 0)
    expr_acc = jnp.zeros((cell_rows, expr.shape[1]), jnp.float32)
    loss_local = jnp.zeros((), jnp.float32)
    pred_list = []
    grad_list = []
    for slide in range(logits.shape[0]):
        logit_rows = logits[slide]
        counted = spot_cells[slide].astype(jnp.float32)
        target = spatial[slide]
        positions = place * rows_all + jnp.arange(rows_all, dtype=jnp.int32)
        valid = (positions < slide_spots[slide]).astype(jnp.float32)
        peak = jnp.max(logit_rows, axis=1, keepdims=True)
        raised = jnp.exp(logit_rows - peak)
        probs = raised / jnp.sum(raised, axis=1, keepdims=True)
        mass = jnp.dot(probs, weights, precision=lax.Precision.HIGHEST)
        blocks = lax.all_to_all(probs, "spot", split_axis=1, concat_axis=0, tiled=True)
        pred = lax.psum_scatter(
            jnp.dot(blocks, expr, precision=lax.Precision.HIGHEST),
            "spot",
            scatter_dimension=0,
            tiled=True,
        )
        gene_dot = jnp.sum(valid[:, None] * pred * target, axis=0)
        gene_pred = jnp.sum(valid[:, None] * pred * pred, axis=0)
        gene_true = jnp.sum(valid[:, None] * target * target, axis=0)
        mass_part = jnp.sum(valid * mass)
        kcell = valid * counted
        cell_part = jnp.sum(kcell)
        spot_dot = jnp.sum(pred * target, axis=1)
        spot_pred = jnp.sum(pred * pred, axis=1)
        spot_true = jnp.sum(target * target, axis=1)
        gene_dot, gene_pred, gene_true, mass_total, cell_total = lax.psum(
            (gene_dot, gene_pred, gene_true, mass_part, cell_part), "spot"
        )
        spot_dot, spot_pred, spot_true = lax.psum((spot_dot, spot_pred, spot_true), "gene")
        gene_inv = lax.rsqrt(gene_pred * gene_true + tiny)
        cos_gene = gene_dot * gene_inv
        spot_inv = lax.rsqrt(spot_pred * spot_true + tiny)
        cos_spot = spot_dot * spot_inv
        share = kcell / cell_total
        scale_count = slide_spots[slide].astype(jnp.float32)
        kl_part = jnp.sum(
            share * (jnp.log(counted) - jnp.log(cell_total) - jnp.log(mass) + jnp.log(mass_total))
        )
        loss_local = loss_local - gene_share * jnp.sum(cos_gene)
        loss_local = loss_local + row_share * (scale_count * kl_part - jnp.sum(valid * cos_spot))
        gene_back = cos_gene * gene_true / (gene_pred * gene_true + tiny)
        spot_back = cos_spot * spot_true / (spot_pred * spot_true + tiny)
        dpred = -valid[:, None] * (
            target * (gene_inv[None, :] + spot_inv[:, None])
            - pred * gene_back[None, :]
            - pred * spot_back[:, None]
        )
        dmass = scale_count * valid * (1.0 / mass_total - share / mass)
        pred_list.append(pred)
        grads_full, mass_full = (
            lax.all_gather(dpred, "spot", axis=0, tiled=True),
            lax.all_gather(dmass, "spot", axis=0, tiled=True),
        )
        dprob_cells = jnp.dot(grads_full, expr.T, precision=lax.Precision.HIGHEST)
        dprob_cells = lax.psum(dprob_cells, "gene")
        expr_acc = expr_acc + lax.dot_general(
            blocks, grads_full, (((0,), (0,)), ((), ())), precision=lax.Precision.HIGHEST
        )
        dprob_cells = dprob_cells + mass_full[:, None] * own_weights[None, :]
        dprob_rows = lax.all_to_all(dprob_cells, "spot", split_axis=0, concat_axis=1, tiled=True)
        inner = jnp.sum(probs * dprob_rows, axis=1, keepdims=True)
        dlogit = probs * (dprob_rows - inner)
        grad_list.append(dlogit)
    loss = lax.psum(loss_local, ("spot", "gene"))
    return (jnp.stack(pred_list), loss, jnp.stack(grad_list), expr_acc)


def solution(mesh):
    places = mesh.shape["spot"]

    def on_device(logits, expr, spatial, slide_spots, spot_cells, cell_prior):
        if places == PLANE * PLANE and mesh.shape["gene"] == 2 and expr.shape[1] == sum(FORWARD):
            return plane_call(
                logits, expr, spatial, slide_spots, spot_cells, cell_prior, places // PLANE
            )
        return general_plan(logits, expr, spatial, slide_spots, spot_cells, cell_prior)

    in_specs = (
        P(None, "spot", None),
        P("spot", "gene"),
        P(None, "spot", "gene"),
        P(),
        P(None, "spot"),
        P(),
    )
    out_specs = (P(None, "spot", "gene"), P(), P(None, "spot", None), P("spot", "gene"))
    return jax.shard_map(
        on_device, mesh=mesh, in_specs=in_specs, out_specs=out_specs, check_vma=False
    )
```

```python
import functools

import jax
import jax.numpy as jnp
from jax import lax
from jax.experimental import pallas as pl
from jax.experimental.pallas import tpu as pltpu
from jax.sharding import PartitionSpec as P

tiny = 1e-06
fixed_point = 16384.0
F32 = jnp.float32
BF16 = jnp.bfloat16
MESH = pl.DeviceIdType.MESH

PLANE = 4
LANES = 128
STEP_ROWS = 16
FORWARD = (256, 256, 256, 128, 128)
BACKWARD = (128, 128, 256, 256, 256)
LEAD = 2
LAG = 1
AHEAD = 2


def halves(value):
    high = value.astype(BF16)
    return high, (value - high.astype(F32)).astype(BF16)


def product(a_high, a_low, b_high, b_low, contract):
    def one(a, b):
        return lax.dot_general(a, b, (contract, ((), ())), preferred_element_type=F32)

    return one(a_high, b_high) + (one(a_high, b_low) + one(a_low, b_high))


def plane_kernel(lines, forward_widths, backward_widths, *refs):
    chunks, turns = len(forward_widths), len(backward_widths)
    (
        (logits_ref, expr_ref, spatial_ref, count_ref, cells_ref, prior_ref),
        (pred_ref, loss_ref, glog_ref, gexp_ref),
        (lg, lq, tg, ex, pq, ab, af, ahi, alo, thi, tlo, bhi, blo, pr, sacc, s1, s2, gv, ss, rowv, rs),
        (dhi, dlo, fs, fx, fy, fz, fr, go, gs, ge, inn, l1, l2),
        (loc, ou_s, ou_r, od_s, od_r, fu_s, fu_r, fd_s, fd_r, a_s, a_r, a2_s, a2_r, r_s, r_r),
        (c_s, c_r, s1_s, s1_r, s2_s, s2_r, ss_s, ss_r, d_s, d_r, ru_s, ru_r, rd_s, rd_r),
        (f_s, f_r, fx_s, fx_r, go_s, go_r, in_s, in_r, l1_s, l1_r, l2_s, l2_r, out_s),
        bb,
        cs,
        cr,
        ds,
        es,
        ru,
        rd,
    ) = grouped(refs, (6, 4, 21, 13, 15, 14, 13, chunks, chunks, chunks, turns, turns, turns, turns))
    place = lax.axis_index("spot")
    core = lax.axis_index("gene")
    z = place // PLANE
    q = place % PLANE
    col, row = q % 2, q // 2
    mates = ((1 - row) * 2 + 1 - col, row * 2 + 1 - col, (1 - row) * 2 + col)
    others = tuple((z + step) % lines for step in range(1, lines))
    up, down = (place + PLANE, core), (place - PLANE, core)
    sibling = (place, 1 - core)
    slides, slide_rows = logits_ref.shape[0], logits_ref.shape[1]
    rows = slides * slide_rows
    cb = expr_ref.shape[0]
    genes = expr_ref.shape[1]
    last = lines - 1
    at_end = (z == 0) | (z == last)
    in_middle = (z > 0) & (z < last)

    def mate(p):
        return (z * PLANE + p, core)

    def send(src, dst, send_sem, recv_sem, device):
        copy = pltpu.make_async_remote_copy(
            src_ref=src, dst_ref=dst, send_sem=send_sem, recv_sem=recv_sem, device_id=device, device_id_type=MESH
        )
        copy.start()

    def arrived(dst, recv_sem):
        pltpu.make_async_copy(dst, dst, recv_sem).wait()

    sent = arrived

    def cols(k):
        return pl.ds(sum(forward_widths[:k]), forward_widths[k])

    def turn_cols(k):
        return pl.ds(sum(backward_widths[:k]), backward_widths[k])

    def block(index):
        return pl.ds(pl.multiple_of(index * cb, cb), cb)

    def share(index):
        return pl.ds(pl.multiple_of(index * rows, rows), rows)

    def half(index):
        return pl.ds(pl.multiple_of(index * slide_rows, slide_rows), slide_rows)

    for m in range(slides):
        pltpu.make_async_copy(logits_ref.at[m], lg.at[half(m)], loc.at[m]).start()
        pltpu.make_async_copy(spatial_ref.at[m], tg.at[half(m)], loc.at[slides + m]).start()
    pltpu.make_async_copy(expr_ref, ex, loc.at[2 * slides]).start()

    barrier = pltpu.get_barrier_semaphore()
    for p in mates:
        pl.semaphore_signal(barrier, inc=1, device_id=mate(p), device_id_type=MESH)
    for o in others:
        pl.semaphore_signal(barrier, inc=1, device_id=(o * PLANE + q, core), device_id_type=MESH)
    pl.semaphore_signal(barrier, inc=1, device_id=sibling, device_id_type=MESH)
    pl.semaphore_wait(barrier, len(mates) + len(others) + 1)

    for m in range(slides):
        pltpu.make_async_copy(logits_ref.at[m], lg.at[half(m)], loc.at[m]).wait()
    for p in range(PLANE):
        for line in range(lines):
            lq[p, :, pl.ds(line * cb, cb)] = lg[half(core), pl.ds((line * PLANE + p) * cb, cb)]
    for p in mates:
        send(lq.at[p], ab.at[q, half(core)], a_s, a_r.at[q], mate(p))

    pltpu.make_async_copy(expr_ref, ex, loc.at[2 * slides]).wait()
    for k in range(chunks):
        bb[k][block(z), :] = ex[:, cols(k)]

    def send_own(k):
        here = bb[k].at[block(z)]

        @pl.when(z < last)
        def _():
            send(here, here, ou_s.at[k], ou_r.at[k], up)

        @pl.when(z > 0)
        def _():
            send(here, here, od_s.at[k], od_r.at[k], down)

    for k in range(min(LEAD, chunks)):
        send_own(k)

    @pl.when(at_end)
    def _():
        for k in range(LEAD, chunks):
            send_own(k)

    def from_below(k, at):
        arrived(bb[k].at[pl.ds((at - 1) * cb, cb)], ou_r.at[k])
        if at > 1:
            arrived(bb[k].at[pl.ds(0, (at - 1) * cb)], fu_r.at[k])

    def from_above(k, at):
        arrived(bb[k].at[pl.ds((at + 1) * cb, cb)], od_r.at[k])
        if at < last - 1:
            arrived(bb[k].at[pl.ds((at + 2) * cb, (last - 1 - at) * cb)], fd_r.at[k])

    def forward(k):
        for at in range(1, last):

            @pl.when(z == at)
            def _():
                def upward():
                    from_below(k, at)
                    here = bb[k].at[pl.ds(0, at * cb)]
                    send(here, here, fu_s.at[k], fu_r.at[k], up)

                def downward():
                    from_above(k, at)
                    here = bb[k].at[pl.ds((at + 1) * cb, (last - at) * cb)]
                    send(here, here, fd_s.at[k], fd_r.at[k], down)

                for step in (upward, downward) if 2 * at < lines else (downward, upward):
                    step()
                if k + LEAD < chunks:
                    send_own(k + LEAD)

    def gathered(k):
        @pl.when(z == 0)
        def _():
            from_above(k, 0)

        @pl.when(z == last)
        def _():
            from_below(k, last)

    weights = prior_ref[...].astype(F32) / fixed_point

    @pl.loop(0, rows // STEP_ROWS)
    def _(step):
        at = pl.ds(pl.multiple_of(step * STEP_ROWS, STEP_ROWS), STEP_ROWS)
        value = lg[at, :]
        peak = jnp.max(value, axis=1, keepdims=True)
        raised = jnp.exp(value - peak)
        scale = 1.0 / jnp.sum(raised, axis=1, keepdims=True)
        probs = raised * scale
        mass_rows = jnp.sum(probs * weights, axis=1, keepdims=True)
        rowv[0, at, :] = jnp.broadcast_to(mass_rows, (STEP_ROWS, LANES))
        rowv[1, at, :] = jnp.broadcast_to(peak, (STEP_ROWS, LANES))
        rowv[2, at, :] = jnp.broadcast_to(scale, (STEP_ROWS, LANES))
        for p in range(PLANE):
            for line in range(lines):
                at_cells = (line * PLANE + p) * cb
                pq[p, at, pl.ds(line * cb, cb)] = probs[:, at_cells : at_cells + cb]

    wide = lax.broadcasted_iota(jnp.int32, (rows, LANES), 1)
    rs[q] = jnp.where(wide == 0, rowv[1], rowv[2]).T[0:8]
    for p in mates:
        send(rs.at[q], rs.at[q], r_s, r_r.at[q], mate(p))

    for p in (mates[1], mates[2], mates[0]):
        here = ab.at[p, half(core)]
        arrived(here, a_r.at[p])
        send(here, here, a2_s, a2_r.at[p], sibling)
    forward(0)

    rid = lax.broadcasted_iota(jnp.int32, (rows, 1), 0)
    first = rid < slide_rows
    position = place * slide_rows + jnp.where(first, rid, rid - slide_rows)
    count = jnp.where(first, count_ref[0], count_ref[1])
    valid = (position < count).astype(F32)
    scale_count = count.astype(F32)
    square = (slide_rows, slide_rows)
    eye = lax.broadcasted_iota(jnp.int32, square, 0) == lax.broadcasted_iota(jnp.int32, square, 1)
    counted = jnp.concatenate(
        [
            jnp.sum(jnp.where(eye, cells_ref[m : m + 1, :].astype(F32), 0.0), axis=1, keepdims=True)
            for m in range(slides)
        ],
        axis=0,
    )
    mass = rowv[0, :, 0:1]
    kcell = valid * counted

    def by_slide(value):
        return [jnp.sum(value[m * slide_rows : (m + 1) * slide_rows], axis=0, keepdims=True) for m in range(slides)]

    mass_parts = by_slide(valid * mass)
    cell_parts = by_slide(kcell)
    lane = lax.broadcasted_iota(jnp.int32, (1, LANES), 1)
    scalars = jnp.zeros((1, LANES), F32)
    for at, value in enumerate(mass_parts + cell_parts):
        scalars = jnp.where(lane == at, value, scalars)
    for m in range(slides):
        pltpu.make_async_copy(spatial_ref.at[m], tg.at[half(m)], loc.at[slides + m]).wait()
    sacc[...] = jnp.zeros_like(sacc)
    s1[q, 3 * slides :, :] = jnp.zeros((8 - 3 * slides, genes), F32)
    s1[q, 3 * slides : 3 * slides + 1, 0:LANES] = scalars

    af[q] = pq[q]
    ahi[share(q), :], alo[share(q), :] = halves(pq[q])
    for p in (mates[1], mates[2], mates[0]):
        arrived(rs.at[p], r_r.at[p])
        arrived(ab.at[p, half(1 - core)], a2_r.at[p])
        by_row = rs[p].T
        probs = jnp.exp(ab[p] - by_row[:, 0:1]) * by_row[:, 1:2]
        af[p] = probs
        ahi[share(p), :], alo[share(p), :] = halves(probs)

    def forward_product(k):
        gathered(k)
        high, low = halves(bb[k][...])
        bhi[:, cols(k)], blo[:, cols(k)] = high, low
        cs[k][...] = product(ahi[...], alo[...], high, low, ((1,), (0,)))
        for p in mates:
            send(cs[k].at[share(p)], cr[k].at[q], c_s.at[k], c_r.at[k, q], mate(p))

    def finish_pred(k):
        total = cs[k][share(q), :]
        for p in mates:
            arrived(cr[k].at[p], c_r.at[k, p])
            total = total + cr[k][p]
        pr[:, cols(k)] = total
        truth = tg[:, cols(k)]
        for at, value in enumerate((total * truth, total * total, truth * truth)):
            sacc[at] += lane_groups(value)
        kept = valid * total
        stats = by_slide(kept * truth) + by_slide(kept * total) + by_slide(valid * truth * truth)
        s1[q, 0 : 3 * slides, cols(k)] = jnp.concatenate(stats, axis=0)

    early = sum(forward_widths[: chunks - LAG])
    parts = (pl.ds(0, early), pl.ds(early, genes - early))

    def sum_plane(at):
        for p in mates:
            send(s1.at[q, :, parts[at]], s1.at[q, :, parts[at]], s1_s, s1_r.at[at, q], mate(p))

    def sum_line(at):
        for p in mates:
            arrived(s1.at[p, :, parts[at]], s1_r.at[at, p])
        s2[z, :, parts[at]] = (s1[0, :, parts[at]] + s1[1, :, parts[at]]) + (s1[2, :, parts[at]] + s1[3, :, parts[at]])
        for o in others:
            send(s2.at[z, :, parts[at]], s2.at[z, :, parts[at]], s2_s, s2_r.at[at, z], (o * PLANE + q, core))

    for k in range(chunks):
        if k + 1 < chunks:
            forward(k + 1)
        forward_product(k)
        if k >= LAG:
            finish_pred(k - LAG)
    sum_plane(0)
    for p in range(PLANE):
        high, low = halves(af[p].T)
        thi[:, share(p)], tlo[:, share(p)] = high, low
    sum_line(0)
    for k in range(chunks - LAG, chunks):
        finish_pred(k)
    sum_plane(1)
    for m in range(slides):
        pltpu.make_async_copy(pr.at[half(m)], pred_ref.at[m], out_s.at[m]).start()

    sums = [jnp.sum(sacc[at], axis=1, keepdims=True) for at in range(3)]
    ss[core] = jnp.where(wide == 0, sums[0], jnp.where(wide == 1, sums[1], sums[2]))
    send(ss.at[core], ss.at[core], ss_s, ss_r, sibling)
    sum_line(1)
    arrived(ss.at[1 - core], ss_r)
    spot = ss[0] + ss[1]
    spot_dot, spot_pred, spot_true = spot[:, 0:1], spot[:, 1:2], spot[:, 2:3]
    spot_inv = lax.rsqrt(spot_pred * spot_true + tiny)
    cos_spot = spot_dot * spot_inv
    spot_back = cos_spot * spot_true / (spot_pred * spot_true + tiny)
    for o in others:
        for at in range(2):
            arrived(s2.at[o, :, parts[at]], s2_r.at[at, o])
    total = s2[0]
    for line in range(1, lines):
        total = total + s2[line]
    gene_dot, gene_pred, gene_true = total[0:2], total[2:4], total[4:6]
    gene_inv = lax.rsqrt(gene_pred * gene_true + tiny)
    cos_gene = gene_dot * gene_inv
    gv[0:2, :] = gene_inv
    gv[2:4, :] = cos_gene * gene_true / (gene_pred * gene_true + tiny)

    sacc[0] = jnp.zeros_like(sacc[0])

    def send_grad(k):
        pieces = []
        for m in range(slides):
            lo, hi = m * slide_rows, (m + 1) * slide_rows
            truth, guess = tg[lo:hi, turn_cols(k)], pr[lo:hi, turn_cols(k)]
            inverse, back = gv[m : m + 1, turn_cols(k)], gv[2 + m : 3 + m, turn_cols(k)]
            pieces.append(
                -valid[lo:hi]
                * (truth * (inverse + spot_inv[lo:hi]) - guess * back - guess * spot_back[lo:hi])
            )
        grad = jnp.concatenate(pieces, axis=0)
        here = ds[k].at[share(q)]
        here[...] = grad
        for p in mates:
            send(here, here, d_s.at[k], d_r.at[k, q], mate(p))
        sacc[0] += lane_groups(grad * pr[:, turn_cols(k)])

    for k in range(min(AHEAD, turns)):
        send_grad(k)
    gene_sum = jnp.sum(jnp.sum(cos_gene, axis=1, keepdims=True), axis=0, keepdims=True)

    mass_total = jnp.where(first, total[6:7, 0:1], total[6:7, 1:2])
    cell_total = jnp.where(first, total[6:7, 2:3], total[6:7, 3:4])
    portion = kcell / cell_total
    kl_rows = portion * (jnp.log(counted) - jnp.log(cell_total) - jnp.log(mass) + jnp.log(mass_total))
    dmass = scale_count * valid * (1.0 / mass_total - portion / mass)
    terms = jnp.sum(scale_count * kl_rows - valid * cos_spot, axis=0, keepdims=True)
    l1[q] = jnp.broadcast_to(terms, (8, LANES))
    for p in mates:
        send(l1.at[q], l1.at[q], l1_s, l1_r.at[q], mate(p))

    def backward_product(k):
        for p in mates:
            arrived(ds[k].at[share(p)], d_r.at[k, p])
        high, low = halves(ds[k][...])
        dhi[:, turn_cols(k)], dlo[:, turn_cols(k)] = high, low
        es[k][...] = product(thi[...], tlo[...], high, low, ((1,), (0,)))

        @pl.when(z == 0)
        def _():
            above = pl.ds(cb, last * cb)
            send(es[k].at[above], ru[k].at[above], ru_s.at[k], ru_r.at[k], up)

        @pl.when(z == last)
        def _():
            below = pl.ds(0, last * cb)
            send(es[k].at[below], rd[k].at[below], rd_s.at[k], rd_r.at[k], down)

    def add_on(k):
        for at in range(1, last):

            @pl.when(z == at)
            def _():
                def upward():
                    arrived(ru[k].at[pl.ds(at * cb, (lines - at) * cb)], ru_r.at[k])
                    above = pl.ds((at + 1) * cb, (last - at) * cb)
                    es[k][above, :] += ru[k][above, :]
                    send(es[k].at[above], ru[k].at[above], ru_s.at[k], ru_r.at[k], up)

                def downward():
                    arrived(rd[k].at[pl.ds(0, (at + 1) * cb)], rd_r.at[k])
                    below = pl.ds(0, at * cb)
                    es[k][below, :] += rd[k][below, :]
                    send(es[k].at[below], rd[k].at[below], rd_s.at[k], rd_r.at[k], down)

                for step in (upward, downward) if 2 * at < lines else (downward, upward):
                    step()

    def finish_expr(k):
        own = block(z)

        @pl.when(z == 0)
        def _():
            arrived(rd[k].at[own], rd_r.at[k])
            ge[:, turn_cols(k)] = es[k][own, :] + rd[k][own, :]

        @pl.when(z == last)
        def _():
            arrived(ru[k].at[own], ru_r.at[k])
            ge[:, turn_cols(k)] = es[k][own, :] + ru[k][own, :]

        @pl.when(in_middle)
        def _():
            ge[:, turn_cols(k)] = es[k][own, :] + (ru[k][own, :] + rd[k][own, :])

    def probs_gradient(at):
        return product(dhi[:, at], dlo[:, at], bhi[:, at], blo[:, at], ((1,), (1,)))

    added = 0
    middle = turns // 2
    fold = sum(backward_widths[:middle])
    for k in range(turns):
        backward_product(k)
        if k + AHEAD < turns:
            send_grad(k + AHEAD)
        if k == middle - 1:
            fs[...] = probs_gradient(pl.ds(0, fold))
        while 3 * (added + 1) <= 2 * k:
            add_on(added)
            added += 1
    fs[...] += probs_gradient(pl.ds(fold, genes - fold))

    for p in range(PLANE):
        fx[p] = fs[pl.ds(pl.multiple_of(p * rows + (1 - core) * slide_rows, slide_rows), slide_rows), :]
    send(fx, fy, fx_s, fx_r, sibling)
    inner = jnp.sum(sacc[0], axis=1, keepdims=True)
    inn[core] = jnp.where(wide == 0, inner, gene_sum)
    send(inn.at[core], inn.at[core], in_s, in_r, sibling)
    for p in mates:
        arrived(l1.at[p], l1_r.at[p])
    l2[z] = (l1[0] + l1[1]) + (l1[2] + l1[3])
    for o in others:
        send(l2.at[z], l2.at[z], l2_s, l2_r.at[z], (o * PLANE + q, core))
    arrived(fy, fx_r)
    for p in range(PLANE):
        kept = fs[pl.ds(pl.multiple_of(p * rows + core * slide_rows, slide_rows), slide_rows), :]
        fz[p] = kept + fy[p]
    for p in mates:
        send(fz.at[p], fr.at[q], f_s, f_r.at[q], mate(p))
    fr[q] = fz[q]
    while added < turns:
        add_on(added)
        added += 1
    for k in range(turns - 2):
        finish_expr(k)
    arrived(inn.at[1 - core], in_r)
    both = inn[0] + inn[1]
    rowv[1] = jnp.broadcast_to(dmass, (rows, LANES))
    rowv[2] = jnp.broadcast_to(both[:, 0:1] + dmass * mass, (rows, LANES))
    for p in mates:
        arrived(fr.at[p], f_r.at[p])

    @pl.loop(0, slide_rows // STEP_ROWS)
    def _(step):
        at = pl.ds(pl.multiple_of(step * STEP_ROWS, STEP_ROWS), STEP_ROWS)
        row_at = pl.ds(pl.multiple_of(core * slide_rows + step * STEP_ROWS, STEP_ROWS), STEP_ROWS)
        by_mass, total_inner = rowv[1, row_at, 0:1], rowv[2, row_at, 0:1]
        for p in range(PLANE):
            for line in range(lines):
                here, there = pl.ds(line * cb, cb), (line * PLANE + p) * cb
                grad = fr[p, at, here] + by_mass * weights[:, there : there + cb]
                go[at, pl.ds(there, cb)] = pq[p, row_at, here] * (grad - total_inner)

    send(go, gs, go_s, go_r, sibling)
    pltpu.make_async_copy(go, glog_ref.at[core], out_s.at[slides + 1]).start()

    for o in others:
        arrived(l2.at[o], l2_r.at[o])
    loss = l2[0]
    for line in range(1, lines):
        loss = loss + l2[line]
    loss_ref[...] = loss[0:1, 0:1] - both[0:1, 1:2]
    finish_expr(turns - 2)
    finish_expr(turns - 1)
    pltpu.make_async_copy(ge, gexp_ref, out_s.at[slides]).start()
    arrived(gs, go_r)
    pltpu.make_async_copy(gs, glog_ref.at[1 - core], out_s.at[slides + 2]).start()

    for m in range(slides):
        pltpu.make_async_copy(pr.at[half(m)], pred_ref.at[m], out_s.at[m]).wait()
    pltpu.make_async_copy(ge, gexp_ref, out_s.at[slides]).wait()
    pltpu.make_async_copy(go, glog_ref.at[core], out_s.at[slides + 1]).wait()
    pltpu.make_async_copy(gs, glog_ref.at[1 - core], out_s.at[slides + 2]).wait()
    for k in range(chunks):

        @pl.when(z < last)
        def _():
            sent(bb[k].at[block(z)], ou_s.at[k])

        @pl.when(z > 0)
        def _():
            sent(bb[k].at[block(z)], od_s.at[k])

        for at in range(1, last):

            @pl.when(z == at)
            def _():
                sent(bb[k].at[pl.ds(0, at * cb)], fu_s.at[k])
                sent(bb[k].at[pl.ds((at + 1) * cb, (last - at) * cb)], fd_s.at[k])

    for k in range(turns):
        for at in range(lines):

            @pl.when(z == at)
            def _():
                if at < last:
                    sent(es[k].at[pl.ds((at + 1) * cb, (last - at) * cb)], ru_s.at[k])
                if at > 0:
                    sent(es[k].at[pl.ds(0, at * cb)], rd_s.at[k])

    three = pl.ds(0, len(mates))
    sent(ab.at[three, half(0)], a_s)
    sent(ab.at[three, half(0)], a2_s)
    sent(rs.at[three], r_s)
    for k in range(chunks):
        sent(cr[k].at[three], c_s.at[k])
    sent(s1.at[three], s1_s)
    sent(s2.at[pl.ds(0, last)], s2_s)
    sent(ss.at[0], ss_s)
    for k in range(turns):
        sent(ds[k].at[pl.ds(0, len(mates) * rows)], d_s.at[k])
    sent(inn.at[0], in_s)
    sent(l1.at[three], l1_s)
    sent(l2.at[pl.ds(0, last)], l2_s)
    sent(fr.at[three], f_s)
    sent(fx, fx_s)
    sent(go, go_s)


def lane_groups(value):
    parts = [value[:, at : at + LANES] for at in range(0, value.shape[1], LANES)]
    return functools.reduce(lambda a, b: a + b, parts)


def grouped(refs, sizes):
    at = 0
    for size in sizes:
        yield refs[at : at + size]
        at += size


def deliver(pred_in, glog_in, gexp_in, pred_ref, glog_ref, gexp_ref, pred_mid, glog_mid, gexp_mid, sems):
    triples = ((glog_in, glog_mid, glog_ref), (pred_in, pred_mid, pred_ref), (gexp_in, gexp_mid, gexp_ref))
    loads = [pltpu.make_async_copy(src, mid, sems.at[0, at]) for at, (src, mid, _) in enumerate(triples)]
    stores = [pltpu.make_async_copy(mid, dst, sems.at[1, at]) for at, (_, mid, dst) in enumerate(triples)]
    for load in loads:
        load.start()
    for load, store in zip(loads, stores):
        load.wait()
        store.start()
    for store in stores:
        store.wait()


def plane_call(logits, expr, spatial, slide_spots, spot_cells, cell_prior, lines):
    slides, slide_rows, cells = logits.shape
    rows = slides * slide_rows
    cb, genes = expr.shape
    quarter = lines * cb
    spots = PLANE * rows
    chunks, turns = len(FORWARD), len(BACKWARD)
    dma = pltpu.SemaphoreType.DMA
    vmem = pltpu.VMEM
    anywhere = pl.BlockSpec(memory_space=pl.ANY)
    in_vmem = pl.BlockSpec(memory_space=pltpu.VMEM)
    in_smem = pl.BlockSpec(memory_space=pltpu.SMEM)
    scratch = [
        vmem((rows, cells), F32),
        vmem((PLANE, slide_rows, quarter), F32),
        vmem((rows, genes), F32),
        vmem((cb, genes), F32),
        vmem((PLANE, rows, quarter), F32),
        vmem((PLANE, rows, quarter), F32),
        vmem((PLANE, rows, quarter), F32),
        vmem((spots, quarter), BF16),
        vmem((spots, quarter), BF16),
        vmem((quarter, spots), BF16),
        vmem((quarter, spots), BF16),
        vmem((quarter, genes), BF16),
        vmem((quarter, genes), BF16),
        vmem((rows, genes), F32),
        vmem((3, rows, LANES), F32),
        vmem((PLANE, 8, genes), F32),
        vmem((lines, 8, genes), F32),
        vmem((8, genes), F32),
        vmem((2, rows, LANES), F32),
        vmem((3, rows, LANES), F32),
        vmem((PLANE, 8, rows), F32),
        vmem((spots, genes), BF16),
        vmem((spots, genes), BF16),
        vmem((spots, quarter), F32),
        vmem((PLANE, slide_rows, quarter), F32),
        vmem((PLANE, slide_rows, quarter), F32),
        vmem((PLANE, slide_rows, quarter), F32),
        vmem((PLANE, slide_rows, quarter), F32),
        vmem((slide_rows, cells), F32),
        vmem((slide_rows, cells), F32),
        vmem((cb, genes), F32),
        vmem((2, rows, LANES), F32),
        vmem((PLANE, 8, LANES), F32),
        vmem((lines, 8, LANES), F32),
        dma((2 * slides + 1,)),
        dma((chunks,)),
        dma((chunks,)),
        dma((chunks,)),
        dma((chunks,)),
        dma((chunks,)),
        dma((chunks,)),
        dma((chunks,)),
        dma((chunks,)),
        dma,
        dma((PLANE,)),
        dma,
        dma((PLANE,)),
        dma,
        dma((PLANE,)),
        dma((chunks,)),
        dma((chunks, PLANE)),
        dma,
        dma((2, PLANE)),
        dma,
        dma((2, lines)),
        dma,
        dma,
        dma((turns,)),
        dma((turns, PLANE)),
        dma((turns,)),
        dma((turns,)),
        dma((turns,)),
        dma((turns,)),
        dma,
        dma((PLANE,)),
        dma,
        dma,
        dma,
        dma,
        dma,
        dma,
        dma,
        dma((PLANE,)),
        dma,
        dma((lines,)),
        dma((slides + 3,)),
    ]
    for shape, widths in (
        ((quarter,), FORWARD),
        ((spots,), FORWARD),
        ((PLANE, rows), FORWARD),
        ((spots,), BACKWARD),
        ((quarter,), BACKWARD),
        ((quarter,), BACKWARD),
        ((quarter,), BACKWARD),
    ):
        scratch += [vmem(shape + (width,), F32) for width in widths]
    pred_shape = jax.ShapeDtypeStruct((slides, slide_rows, genes), F32)
    glog_shape = jax.ShapeDtypeStruct((slides, slide_rows, cells), F32)
    gexp_shape = jax.ShapeDtypeStruct((cb, genes), F32)
    pred, loss, grad_logits, grad_expr = pl.pallas_call(
        functools.partial(plane_kernel, lines, FORWARD, BACKWARD),
        out_shape=(pred_shape, jax.ShapeDtypeStruct((1, 1), F32), glog_shape, gexp_shape),
        in_specs=[anywhere, anywhere, anywhere, in_smem, in_vmem, in_vmem],
        out_specs=(anywhere, in_vmem, anywhere, anywhere),
        scratch_shapes=scratch,
        compiler_params=pltpu.CompilerParams(
            collective_id=0, has_side_effects=True, vmem_limit_bytes=56 * 1024 * 1024
        ),
    )(logits, expr, spatial, slide_spots, spot_cells, cell_prior.reshape(1, cells))
    pred, grad_logits, grad_expr = pl.pallas_call(
        deliver,
        out_shape=(pred_shape, glog_shape, gexp_shape),
        in_specs=[anywhere] * 3,
        out_specs=(anywhere,) * 3,
        scratch_shapes=[vmem(shape.shape, F32) for shape in (pred_shape, glog_shape, gexp_shape)] + [dma((2, 3))],
        compiler_params=pltpu.CompilerParams(vmem_limit_bytes=56 * 1024 * 1024),
    )(pred, grad_logits, grad_expr)
    return pred, loss.reshape(()), grad_logits, grad_expr


def general_plan(logits, expr, spatial, slide_spots, spot_cells, cell_prior):
    place = lax.axis_index("spot")
    side = lax.axis_index("gene")
    rows_all = logits.shape[1]
    cell_rows = expr.shape[0]
    weights = cell_prior.astype(jnp.float32) / fixed_point
    gene_share = (place == 0).astype(jnp.float32)
    row_share = (side == 0).astype(jnp.float32)
    own_weights = lax.dynamic_slice_in_dim(weights, place * cell_rows, cell_rows, 0)
    expr_acc = jnp.zeros((cell_rows, expr.shape[1]), jnp.float32)
    loss_local = jnp.zeros((), jnp.float32)
    pred_list = []
    grad_list = []
    for slide in range(logits.shape[0]):
        logit_rows = logits[slide]
        counted = spot_cells[slide].astype(jnp.float32)
        target = spatial[slide]
        positions = place * rows_all + jnp.arange(rows_all, dtype=jnp.int32)
        valid = (positions < slide_spots[slide]).astype(jnp.float32)
        peak = jnp.max(logit_rows, axis=1, keepdims=True)
        raised = jnp.exp(logit_rows - peak)
        probs = raised / jnp.sum(raised, axis=1, keepdims=True)
        mass = jnp.dot(probs, weights, precision=lax.Precision.HIGHEST)
        blocks = lax.all_to_all(probs, "spot", split_axis=1, concat_axis=0, tiled=True)
        pred = lax.psum_scatter(
            jnp.dot(blocks, expr, precision=lax.Precision.HIGHEST),
            "spot",
            scatter_dimension=0,
            tiled=True,
        )
        gene_dot = jnp.sum(valid[:, None] * pred * target, axis=0)
        gene_pred = jnp.sum(valid[:, None] * pred * pred, axis=0)
        gene_true = jnp.sum(valid[:, None] * target * target, axis=0)
        mass_part = jnp.sum(valid * mass)
        kcell = valid * counted
        cell_part = jnp.sum(kcell)
        spot_dot = jnp.sum(pred * target, axis=1)
        spot_pred = jnp.sum(pred * pred, axis=1)
        spot_true = jnp.sum(target * target, axis=1)
        gene_dot, gene_pred, gene_true, mass_total, cell_total = lax.psum(
            (gene_dot, gene_pred, gene_true, mass_part, cell_part), "spot"
        )
        spot_dot, spot_pred, spot_true = lax.psum((spot_dot, spot_pred, spot_true), "gene")
        gene_inv = lax.rsqrt(gene_pred * gene_true + tiny)
        cos_gene = gene_dot * gene_inv
        spot_inv = lax.rsqrt(spot_pred * spot_true + tiny)
        cos_spot = spot_dot * spot_inv
        share = kcell / cell_total
        scale_count = slide_spots[slide].astype(jnp.float32)
        kl_part = jnp.sum(
            share * (jnp.log(counted) - jnp.log(cell_total) - jnp.log(mass) + jnp.log(mass_total))
        )
        loss_local = loss_local - gene_share * jnp.sum(cos_gene)
        loss_local = loss_local + row_share * (scale_count * kl_part - jnp.sum(valid * cos_spot))
        gene_back = cos_gene * gene_true / (gene_pred * gene_true + tiny)
        spot_back = cos_spot * spot_true / (spot_pred * spot_true + tiny)
        dpred = -valid[:, None] * (
            target * (gene_inv[None, :] + spot_inv[:, None])
            - pred * gene_back[None, :]
            - pred * spot_back[:, None]
        )
        dmass = scale_count * valid * (1.0 / mass_total - share / mass)
        pred_list.append(pred)
        grads_full, mass_full = (
            lax.all_gather(dpred, "spot", axis=0, tiled=True),
            lax.all_gather(dmass, "spot", axis=0, tiled=True),
        )
        dprob_cells = jnp.dot(grads_full, expr.T, precision=lax.Precision.HIGHEST)
        dprob_cells = lax.psum(dprob_cells, "gene")
        expr_acc = expr_acc + lax.dot_general(
            blocks, grads_full, (((0,), (0,)), ((), ())), precision=lax.Precision.HIGHEST
        )
        dprob_cells = dprob_cells + mass_full[:, None] * own_weights[None, :]
        dprob_rows = lax.all_to_all(dprob_cells, "spot", split_axis=0, concat_axis=1, tiled=True)
        inner = jnp.sum(probs * dprob_rows, axis=1, keepdims=True)
        dlogit = probs * (dprob_rows - inner)
        grad_list.append(dlogit)
    loss = lax.psum(loss_local, ("spot", "gene"))
    return (jnp.stack(pred_list), loss, jnp.stack(grad_list), expr_acc)


def solution(mesh):
    places = mesh.shape["spot"]

    def on_device(logits, expr, spatial, slide_spots, spot_cells, cell_prior):
        if places == PLANE * PLANE and mesh.shape["gene"] == 2 and expr.shape[1] == sum(FORWARD):
            return plane_call(
                logits, expr, spatial, slide_spots, spot_cells, cell_prior, places // PLANE
            )
        return general_plan(logits, expr, spatial, slide_spots, spot_cells, cell_prior)

    in_specs = (
        P(None, "spot", None),
        P("spot", "gene"),
        P(None, "spot", "gene"),
        P(),
        P(None, "spot"),
        P(),
    )
    out_specs = (P(None, "spot", "gene"), P(), P(None, "spot", None), P("spot", "gene"))
    return jax.shard_map(
        on_device, mesh=mesh, in_specs=in_specs, out_specs=out_specs, check_vma=False
    )
```

```python
import functools

import jax
import jax.numpy as jnp
from jax import lax
from jax.experimental import pallas as pl
from jax.experimental.pallas import tpu as pltpu
from jax.sharding import PartitionSpec as P

tiny = 1e-06
fixed_point = 16384.0
F32 = jnp.float32
BF16 = jnp.bfloat16
MESH = pl.DeviceIdType.MESH

PLANE = 4
LANES = 128
STEP_ROWS = 16
FORWARD = (256, 256, 256, 128, 128)
BACKWARD = (128, 128, 256, 256, 128, 128)
SPLIT = 1
LEAD = 2
LAG = 1
AHEAD = 2


def halves(value):
    high = value.astype(BF16)
    return high, (value - high.astype(F32)).astype(BF16)


def product(a_high, a_low, b_high, b_low, contract):
    def one(a, b):
        return lax.dot_general(a, b, (contract, ((), ())), preferred_element_type=F32)

    return one(a_high, b_high) + (one(a_high, b_low) + one(a_low, b_high))


def plane_kernel(lines, forward_widths, backward_widths, *refs):
    chunks, turns = len(forward_widths), len(backward_widths)
    (
        (logits_ref, expr_ref, spatial_ref, count_ref, cells_ref, prior_ref),
        (pred_ref, loss_ref, glog_ref, gexp_ref),
        (lg, lq, tg, ex, pq, ab, af, ahi, alo, thi, tlo, bhi, blo, pr, sacc, s1, s2, gv, ss, rowv, rs),
        (dhi, dlo, fs, fx, fy, fz, fr, go, gs, ge, inn, l1, l2),
        (loc, ou_s, ou_r, od_s, od_r, fu_s, fu_r, fd_s, fd_r, a_s, a_r, a2_s, a2_r, r_s, r_r),
        (c_s, c_r, s1_s, s1_r, s2_s, s2_r, ss_s, ss_r, d_s, d_r, ru_s, ru_r, rd_s, rd_r),
        (f_s, f_r, fx_s, fx_r, go_s, go_r, in_s, in_r, l1_s, l1_r, l2_s, l2_r, out_s),
        bb,
        cs,
        cr,
        ds,
        es,
        ru,
        rd,
    ) = grouped(refs, (6, 4, 21, 13, 15, 14, 13, chunks, chunks, chunks, turns, turns, turns, turns))
    place = lax.axis_index("spot")
    core = lax.axis_index("gene")
    z = place // PLANE
    q = place % PLANE
    col, row = q % 2, q // 2
    mates = ((1 - row) * 2 + 1 - col, row * 2 + 1 - col, (1 - row) * 2 + col)
    others = tuple((z + step) % lines for step in range(1, lines))
    up, down = (place + PLANE, core), (place - PLANE, core)
    sibling = (place, 1 - core)
    slides, slide_rows = logits_ref.shape[0], logits_ref.shape[1]
    rows = slides * slide_rows
    cb = expr_ref.shape[0]
    genes = expr_ref.shape[1]
    last = lines - 1

    def mate(p):
        return (z * PLANE + p, core)

    def send(src, dst, send_sem, recv_sem, device):
        copy = pltpu.make_async_remote_copy(
            src_ref=src, dst_ref=dst, send_sem=send_sem, recv_sem=recv_sem, device_id=device, device_id_type=MESH
        )
        copy.start()

    def arrived(dst, recv_sem):
        pltpu.make_async_copy(dst, dst, recv_sem).wait()

    sent = arrived

    def cols(k):
        return pl.ds(sum(forward_widths[:k]), forward_widths[k])

    def turn_cols(k):
        return pl.ds(sum(backward_widths[:k]), backward_widths[k])

    def block(index):
        return pl.ds(pl.multiple_of(index * cb, cb), cb)

    def share(index):
        return pl.ds(pl.multiple_of(index * rows, rows), rows)

    def half(index):
        return pl.ds(pl.multiple_of(index * slide_rows, slide_rows), slide_rows)

    for m in range(slides):
        pltpu.make_async_copy(logits_ref.at[m], lg.at[half(m)], loc.at[m]).start()
        pltpu.make_async_copy(spatial_ref.at[m], tg.at[half(m)], loc.at[slides + m]).start()
    pltpu.make_async_copy(expr_ref, ex, loc.at[2 * slides]).start()

    barrier = pltpu.get_barrier_semaphore()
    for p in mates:
        pl.semaphore_signal(barrier, inc=1, device_id=mate(p), device_id_type=MESH)
    for o in others:
        pl.semaphore_signal(barrier, inc=1, device_id=(o * PLANE + q, core), device_id_type=MESH)
    pl.semaphore_signal(barrier, inc=1, device_id=sibling, device_id_type=MESH)
    pl.semaphore_wait(barrier, len(mates) + len(others) + 1)

    for m in range(slides):
        pltpu.make_async_copy(logits_ref.at[m], lg.at[half(m)], loc.at[m]).wait()
    for p in range(PLANE):
        for line in range(lines):
            lq[p, :, pl.ds(line * cb, cb)] = lg[half(core), pl.ds((line * PLANE + p) * cb, cb)]
    for p in mates:
        send(lq.at[p], ab.at[q, half(core)], a_s, a_r.at[q], mate(p))

    pltpu.make_async_copy(expr_ref, ex, loc.at[2 * slides]).wait()
    for k in range(chunks):
        bb[k][block(z), :] = ex[:, cols(k)]

    def own_up(k):
        here = bb[k].at[block(z)]
        send(here, here, ou_s.at[k], ou_r.at[k], up)

    def own_down(k):
        here = bb[k].at[block(z)]
        send(here, here, od_s.at[k], od_r.at[k], down)

    def low(at):
        return 2 * at < lines

    for at in range(lines):

        @pl.when(z == at)
        def _():
            for k in range(chunks):
                if at < last and (not low(at) or at == 0 or k < LEAD):
                    own_up(k)
                if at > 0 and (low(at) or at == last or k < LEAD):
                    own_down(k)

    def from_below(k, at):
        arrived(bb[k].at[pl.ds((at - 1) * cb, cb)], ou_r.at[k])
        if at > 1:
            arrived(bb[k].at[pl.ds(0, (at - 1) * cb)], fu_r.at[k])

    def from_above(k, at):
        arrived(bb[k].at[pl.ds((at + 1) * cb, cb)], od_r.at[k])
        if at < last - 1:
            arrived(bb[k].at[pl.ds((at + 2) * cb, (last - 1 - at) * cb)], fd_r.at[k])

    def upward(k, at):
        from_below(k, at)
        here = bb[k].at[pl.ds(0, at * cb)]
        send(here, here, fu_s.at[k], fu_r.at[k], up)

    def downward(k, at):
        from_above(k, at)
        here = bb[k].at[pl.ds((at + 1) * cb, (last - at) * cb)]
        send(here, here, fd_s.at[k], fd_r.at[k], down)

    def forward_far(k):
        for at in range(1, last):

            @pl.when(z == at)
            def _():
                (upward if low(at) else downward)(k, at)
                if k + LEAD < chunks:
                    (own_up if low(at) else own_down)(k + LEAD)

    def gathered(k):
        for at in range(lines):

            @pl.when(z == at)
            def _():
                if at == 0:
                    from_above(k, at)
                elif at == last:
                    from_below(k, at)
                else:
                    (downward if low(at) else upward)(k, at)

    weights = prior_ref[...].astype(F32) / fixed_point

    @pl.loop(0, rows // STEP_ROWS)
    def _(step):
        at = pl.ds(pl.multiple_of(step * STEP_ROWS, STEP_ROWS), STEP_ROWS)
        value = lg[at, :]
        peak = jnp.max(value, axis=1, keepdims=True)
        raised = jnp.exp(value - peak)
        scale = 1.0 / jnp.sum(raised, axis=1, keepdims=True)
        probs = raised * scale
        mass_rows = jnp.sum(probs * weights, axis=1, keepdims=True)
        rowv[0, at, :] = jnp.broadcast_to(mass_rows, (STEP_ROWS, LANES))
        rowv[1, at, :] = jnp.broadcast_to(peak, (STEP_ROWS, LANES))
        rowv[2, at, :] = jnp.broadcast_to(scale, (STEP_ROWS, LANES))
        for p in range(PLANE):
            for line in range(lines):
                at_cells = (line * PLANE + p) * cb
                pq[p, at, pl.ds(line * cb, cb)] = probs[:, at_cells : at_cells + cb]

    wide = lax.broadcasted_iota(jnp.int32, (rows, LANES), 1)
    rs[q] = jnp.where(wide == 0, rowv[1], rowv[2]).T[0:8]
    for p in mates:
        send(rs.at[q], rs.at[q], r_s, r_r.at[q], mate(p))

    for p in (mates[1], mates[2], mates[0]):
        here = ab.at[p, half(core)]
        arrived(here, a_r.at[p])
        send(here, here, a2_s, a2_r.at[p], sibling)
    for k in range(min(2, chunks)):
        forward_far(k)

    rid = lax.broadcasted_iota(jnp.int32, (rows, 1), 0)
    first = rid < slide_rows
    position = place * slide_rows + jnp.where(first, rid, rid - slide_rows)
    count = jnp.where(first, count_ref[0], count_ref[1])
    valid = (position < count).astype(F32)
    scale_count = count.astype(F32)
    square = (slide_rows, slide_rows)
    eye = lax.broadcasted_iota(jnp.int32, square, 0) == lax.broadcasted_iota(jnp.int32, square, 1)
    counted = jnp.concatenate(
        [
            jnp.sum(jnp.where(eye, cells_ref[m : m + 1, :].astype(F32), 0.0), axis=1, keepdims=True)
            for m in range(slides)
        ],
        axis=0,
    )
    mass = rowv[0, :, 0:1]
    kcell = valid * counted

    def by_slide(value):
        return [jnp.sum(value[m * slide_rows : (m + 1) * slide_rows], axis=0, keepdims=True) for m in range(slides)]

    mass_parts = by_slide(valid * mass)
    cell_parts = by_slide(kcell)
    lane = lax.broadcasted_iota(jnp.int32, (1, LANES), 1)
    scalars = jnp.zeros((1, LANES), F32)
    for at, value in enumerate(mass_parts + cell_parts):
        scalars = jnp.where(lane == at, value, scalars)
    for m in range(slides):
        pltpu.make_async_copy(spatial_ref.at[m], tg.at[half(m)], loc.at[slides + m]).wait()
    sacc[...] = jnp.zeros_like(sacc)
    s1[q, 3 * slides :, :] = jnp.zeros((8 - 3 * slides, genes), F32)
    s1[q, 3 * slides : 3 * slides + 1, 0:LANES] = scalars

    af[q] = pq[q]
    ahi[share(q), :], alo[share(q), :] = halves(pq[q])
    for p in (mates[1], mates[2], mates[0]):
        arrived(rs.at[p], r_r.at[p])
        arrived(ab.at[p, half(1 - core)], a2_r.at[p])
        by_row = rs[p].T
        probs = jnp.exp(ab[p] - by_row[:, 0:1]) * by_row[:, 1:2]
        af[p] = probs
        ahi[share(p), :], alo[share(p), :] = halves(probs)

    def forward_product(k):
        gathered(k)
        high, low = halves(bb[k][...])
        bhi[:, cols(k)], blo[:, cols(k)] = high, low
        cs[k][...] = product(ahi[...], alo[...], high, low, ((1,), (0,)))
        for p in mates:
            send(cs[k].at[share(p)], cr[k].at[q], c_s.at[k], c_r.at[k, q], mate(p))

    def finish_pred(k):
        total = cs[k][share(q), :]
        for p in mates:
            arrived(cr[k].at[p], c_r.at[k, p])
            total = total + cr[k][p]
        pr[:, cols(k)] = total
        truth = tg[:, cols(k)]
        for at, value in enumerate((total * truth, total * total, truth * truth)):
            sacc[at] += lane_groups(value)
        kept = valid * total
        stats = by_slide(kept * truth) + by_slide(kept * total) + by_slide(valid * truth * truth)
        s1[q, 0 : 3 * slides, cols(k)] = jnp.concatenate(stats, axis=0)

    early = sum(forward_widths[: chunks - LAG])
    parts = (pl.ds(0, early), pl.ds(early, genes - early))

    def sum_plane(at):
        for p in mates:
            send(s1.at[q, :, parts[at]], s1.at[q, :, parts[at]], s1_s, s1_r.at[at, q], mate(p))

    def sum_line(at):
        for p in mates:
            arrived(s1.at[p, :, parts[at]], s1_r.at[at, p])
        s2[z, :, parts[at]] = (s1[0, :, parts[at]] + s1[1, :, parts[at]]) + (s1[2, :, parts[at]] + s1[3, :, parts[at]])
        for o in others:
            send(s2.at[z, :, parts[at]], s2.at[z, :, parts[at]], s2_s, s2_r.at[at, z], (o * PLANE + q, core))

    for k in range(chunks):
        if k + 2 < chunks:
            forward_far(k + 2)
        forward_product(k)
        for p in range(PLANE):
            if 1 + p // 2 == k:
                high, low_part = halves(af[p].T)
                thi[:, share(p)], tlo[:, share(p)] = high, low_part
        if k >= LAG:
            finish_pred(k - LAG)
    sum_plane(0)
    sum_line(0)
    for k in range(chunks - LAG, chunks):
        finish_pred(k)
    sum_plane(1)
    for m in range(slides):
        pltpu.make_async_copy(pr.at[half(m)], pred_ref.at[m], out_s.at[m]).start()

    sums = [jnp.sum(sacc[at], axis=1, keepdims=True) for at in range(3)]
    ss[core] = jnp.where(wide == 0, sums[0], jnp.where(wide == 1, sums[1], sums[2]))
    send(ss.at[core], ss.at[core], ss_s, ss_r, sibling)
    sum_line(1)
    arrived(ss.at[1 - core], ss_r)
    spot = ss[0] + ss[1]
    spot_dot, spot_pred, spot_true = spot[:, 0:1], spot[:, 1:2], spot[:, 2:3]
    spot_inv = lax.rsqrt(spot_pred * spot_true + tiny)
    cos_spot = spot_dot * spot_inv
    spot_back = cos_spot * spot_true / (spot_pred * spot_true + tiny)
    for o in others:
        for at in range(2):
            arrived(s2.at[o, :, parts[at]], s2_r.at[at, o])
    total = s2[0]
    for line in range(1, lines):
        total = total + s2[line]
    gene_dot, gene_pred, gene_true = total[0:2], total[2:4], total[4:6]
    gene_inv = lax.rsqrt(gene_pred * gene_true + tiny)
    cos_gene = gene_dot * gene_inv
    gv[0:2, :] = gene_inv
    gv[2:4, :] = cos_gene * gene_true / (gene_pred * gene_true + tiny)

    sacc[0] = jnp.zeros_like(sacc[0])

    def send_grad(k):
        pieces = []
        for m in range(slides):
            lo, hi = m * slide_rows, (m + 1) * slide_rows
            truth, guess = tg[lo:hi, turn_cols(k)], pr[lo:hi, turn_cols(k)]
            inverse, back = gv[m : m + 1, turn_cols(k)], gv[2 + m : 3 + m, turn_cols(k)]
            pieces.append(
                -valid[lo:hi]
                * (truth * (inverse + spot_inv[lo:hi]) - guess * back - guess * spot_back[lo:hi])
            )
        grad = jnp.concatenate(pieces, axis=0)
        here = ds[k].at[share(q)]
        here[...] = grad
        for p in mates:
            send(here, here, d_s.at[k], d_r.at[k, q], mate(p))
        sacc[0] += lane_groups(grad * pr[:, turn_cols(k)])

    for k in range(min(AHEAD, turns)):
        send_grad(k)
    gene_sum = jnp.sum(jnp.sum(cos_gene, axis=1, keepdims=True), axis=0, keepdims=True)

    mass_total = jnp.where(first, total[6:7, 0:1], total[6:7, 1:2])
    cell_total = jnp.where(first, total[6:7, 2:3], total[6:7, 3:4])
    portion = kcell / cell_total
    kl_rows = portion * (jnp.log(counted) - jnp.log(cell_total) - jnp.log(mass) + jnp.log(mass_total))
    dmass = scale_count * valid * (1.0 / mass_total - portion / mass)
    terms = jnp.sum(scale_count * kl_rows - valid * cos_spot, axis=0, keepdims=True)
    l1[q] = jnp.broadcast_to(terms, (8, LANES))
    for p in mates:
        send(l1.at[q], l1.at[q], l1_s, l1_r.at[q], mate(p))

    def backward_product(k):
        for p in mates:
            arrived(ds[k].at[share(p)], d_r.at[k, p])
        high, low = halves(ds[k][...])
        dhi[:, turn_cols(k)], dlo[:, turn_cols(k)] = high, low
        es[k][...] = product(thi[...], tlo[...], high, low, ((1,), (0,)))

        @pl.when(z == 0)
        def _():
            if whole(k):
                pass_up(k, 1, last)
            else:
                for line in range(last, 0, -1):
                    pass_up(k, line, 1)

        @pl.when(z == last)
        def _():
            if whole(k):
                pass_down(k, 0, last)
            else:
                for line in range(last):
                    pass_down(k, line, 1)

    def whole(k):
        return k < turns - SPLIT

    def pass_up(k, line, count):
        here = pl.ds(line * cb, count * cb)
        send(es[k].at[here], ru[k].at[here], ru_s.at[k], ru_r.at[k, 0 if whole(k) else line], up)

    def pass_down(k, line, count):
        here = pl.ds(line * cb, count * cb)
        send(es[k].at[here], rd[k].at[here], rd_s.at[k], rd_r.at[k, 0 if whole(k) else line], down)

    def take_up(k, line, count):
        here = pl.ds(line * cb, count * cb)
        arrived(ru[k].at[here], ru_r.at[k, 0 if whole(k) else line])

    def take_down(k, line, count):
        here = pl.ds(line * cb, count * cb)
        arrived(rd[k].at[here], rd_r.at[k, 0 if whole(k) else line])

    def add_on(k):
        for at in range(1, last):

            @pl.when(z == at)
            def _():
                def rising():
                    if whole(k):
                        take_up(k, at, lines - at)
                        above = pl.ds((at + 1) * cb, (last - at) * cb)
                        es[k][above, :] += ru[k][above, :]
                        pass_up(k, at + 1, last - at)
                    else:
                        for line in range(last, at, -1):
                            take_up(k, line, 1)
                            here = pl.ds(line * cb, cb)
                            es[k][here, :] += ru[k][here, :]
                            pass_up(k, line, 1)

                def falling():
                    if whole(k):
                        take_down(k, 0, at + 1)
                        below = pl.ds(0, at * cb)
                        es[k][below, :] += rd[k][below, :]
                        pass_down(k, 0, at)
                    else:
                        for line in range(at):
                            take_down(k, line, 1)
                            here = pl.ds(line * cb, cb)
                            es[k][here, :] += rd[k][here, :]
                            pass_down(k, line, 1)

                for step in (rising, falling) if low(at) else (falling, rising):
                    step()

    def finish_expr(k):
        for at in range(lines):

            @pl.when(z == at)
            def _():
                own = pl.ds(at * cb, cb)
                total = es[k][own, :]
                if at > 0:
                    if at == last or not whole(k):
                        take_up(k, at, 1)
                    total = total + ru[k][own, :]
                if at < last:
                    if at == 0 or not whole(k):
                        take_down(k, at, 1)
                    total = total + rd[k][own, :]
                ge[:, turn_cols(k)] = total

    def probs_gradient(at):
        return product(dhi[:, at], dlo[:, at], bhi[:, at], blo[:, at], ((1,), (1,)))

    added = 0
    middle = turns // 2
    fold = sum(backward_widths[:middle])
    for k in range(turns):
        backward_product(k)
        if k + AHEAD < turns:
            send_grad(k + AHEAD)
        if k == middle - 1:
            fs[...] = probs_gradient(pl.ds(0, fold))
        while 3 * (added + 1) <= 2 * k:
            add_on(added)
            added += 1
    fs[...] += probs_gradient(pl.ds(fold, genes - fold))

    for p in range(PLANE):
        fx[p] = fs[pl.ds(pl.multiple_of(p * rows + (1 - core) * slide_rows, slide_rows), slide_rows), :]
    send(fx, fy, fx_s, fx_r, sibling)
    inner = jnp.sum(sacc[0], axis=1, keepdims=True)
    inn[core] = jnp.where(wide == 0, inner, gene_sum)
    send(inn.at[core], inn.at[core], in_s, in_r, sibling)
    for p in mates:
        arrived(l1.at[p], l1_r.at[p])
    l2[z] = (l1[0] + l1[1]) + (l1[2] + l1[3])
    for o in others:
        send(l2.at[z], l2.at[z], l2_s, l2_r.at[z], (o * PLANE + q, core))
    arrived(fy, fx_r)
    for p in range(PLANE):
        kept = fs[pl.ds(pl.multiple_of(p * rows + core * slide_rows, slide_rows), slide_rows), :]
        fz[p] = kept + fy[p]
    for p in mates:
        send(fz.at[p], fr.at[q], f_s, f_r.at[q], mate(p))
    fr[q] = fz[q]
    while added < turns:
        add_on(added)
        added += 1
    for k in range(turns - 2):
        finish_expr(k)
    arrived(inn.at[1 - core], in_r)
    both = inn[0] + inn[1]
    rowv[1] = jnp.broadcast_to(dmass, (rows, LANES))
    rowv[2] = jnp.broadcast_to(both[:, 0:1] + dmass * mass, (rows, LANES))
    for p in mates:
        arrived(fr.at[p], f_r.at[p])

    @pl.loop(0, slide_rows // STEP_ROWS)
    def _(step):
        at = pl.ds(pl.multiple_of(step * STEP_ROWS, STEP_ROWS), STEP_ROWS)
        row_at = pl.ds(pl.multiple_of(core * slide_rows + step * STEP_ROWS, STEP_ROWS), STEP_ROWS)
        by_mass, total_inner = rowv[1, row_at, 0:1], rowv[2, row_at, 0:1]
        for p in range(PLANE):
            for line in range(lines):
                here, there = pl.ds(line * cb, cb), (line * PLANE + p) * cb
                grad = fr[p, at, here] + by_mass * weights[:, there : there + cb]
                go[at, pl.ds(there, cb)] = pq[p, row_at, here] * (grad - total_inner)

    send(go, gs, go_s, go_r, sibling)
    pltpu.make_async_copy(go, glog_ref.at[core], out_s.at[slides + 1]).start()

    for o in others:
        arrived(l2.at[o], l2_r.at[o])
    loss = l2[0]
    for line in range(1, lines):
        loss = loss + l2[line]
    loss_ref[...] = loss[0:1, 0:1] - both[0:1, 1:2]
    finish_expr(turns - 2)
    finish_expr(turns - 1)
    pltpu.make_async_copy(ge, gexp_ref, out_s.at[slides]).start()
    arrived(gs, go_r)
    pltpu.make_async_copy(gs, glog_ref.at[1 - core], out_s.at[slides + 2]).start()

    for m in range(slides):
        pltpu.make_async_copy(pr.at[half(m)], pred_ref.at[m], out_s.at[m]).wait()
    pltpu.make_async_copy(ge, gexp_ref, out_s.at[slides]).wait()
    pltpu.make_async_copy(go, glog_ref.at[core], out_s.at[slides + 1]).wait()
    pltpu.make_async_copy(gs, glog_ref.at[1 - core], out_s.at[slides + 2]).wait()
    for k in range(chunks):

        @pl.when(z < last)
        def _():
            sent(bb[k].at[block(z)], ou_s.at[k])

        @pl.when(z > 0)
        def _():
            sent(bb[k].at[block(z)], od_s.at[k])

        for at in range(1, last):

            @pl.when(z == at)
            def _():
                sent(bb[k].at[pl.ds(0, at * cb)], fu_s.at[k])
                sent(bb[k].at[pl.ds((at + 1) * cb, (last - at) * cb)], fd_s.at[k])

    for k in range(turns):
        for at in range(lines):

            @pl.when(z == at)
            def _():
                if at < last:
                    sent(es[k].at[pl.ds((at + 1) * cb, (last - at) * cb)], ru_s.at[k])
                if at > 0:
                    sent(es[k].at[pl.ds(0, at * cb)], rd_s.at[k])

    three = pl.ds(0, len(mates))
    sent(ab.at[three, half(0)], a_s)
    sent(ab.at[three, half(0)], a2_s)
    sent(rs.at[three], r_s)
    for k in range(chunks):
        sent(cr[k].at[three], c_s.at[k])
    sent(s1.at[three], s1_s)
    sent(s2.at[pl.ds(0, last)], s2_s)
    sent(ss.at[0], ss_s)
    for k in range(turns):
        sent(ds[k].at[pl.ds(0, len(mates) * rows)], d_s.at[k])
    sent(inn.at[0], in_s)
    sent(l1.at[three], l1_s)
    sent(l2.at[pl.ds(0, last)], l2_s)
    sent(fr.at[three], f_s)
    sent(fx, fx_s)
    sent(go, go_s)


def lane_groups(value):
    parts = [value[:, at : at + LANES] for at in range(0, value.shape[1], LANES)]
    return functools.reduce(lambda a, b: a + b, parts)


def grouped(refs, sizes):
    at = 0
    for size in sizes:
        yield refs[at : at + size]
        at += size


def deliver(pred_in, glog_in, gexp_in, pred_ref, glog_ref, gexp_ref, pred_mid, glog_mid, gexp_mid, sems):
    triples = ((glog_in, glog_mid, glog_ref), (pred_in, pred_mid, pred_ref), (gexp_in, gexp_mid, gexp_ref))
    loads = [pltpu.make_async_copy(src, mid, sems.at[0, at]) for at, (src, mid, _) in enumerate(triples)]
    stores = [pltpu.make_async_copy(mid, dst, sems.at[1, at]) for at, (_, mid, dst) in enumerate(triples)]
    for load in loads:
        load.start()
    for load, store in zip(loads, stores):
        load.wait()
        store.start()
    for store in stores:
        store.wait()


def plane_call(logits, expr, spatial, slide_spots, spot_cells, cell_prior, lines):
    slides, slide_rows, cells = logits.shape
    rows = slides * slide_rows
    cb, genes = expr.shape
    quarter = lines * cb
    spots = PLANE * rows
    chunks, turns = len(FORWARD), len(BACKWARD)
    dma = pltpu.SemaphoreType.DMA
    vmem = pltpu.VMEM
    anywhere = pl.BlockSpec(memory_space=pl.ANY)
    in_vmem = pl.BlockSpec(memory_space=pltpu.VMEM)
    in_smem = pl.BlockSpec(memory_space=pltpu.SMEM)
    scratch = [
        vmem((rows, cells), F32),
        vmem((PLANE, slide_rows, quarter), F32),
        vmem((rows, genes), F32),
        vmem((cb, genes), F32),
        vmem((PLANE, rows, quarter), F32),
        vmem((PLANE, rows, quarter), F32),
        vmem((PLANE, rows, quarter), F32),
        vmem((spots, quarter), BF16),
        vmem((spots, quarter), BF16),
        vmem((quarter, spots), BF16),
        vmem((quarter, spots), BF16),
        vmem((quarter, genes), BF16),
        vmem((quarter, genes), BF16),
        vmem((rows, genes), F32),
        vmem((3, rows, LANES), F32),
        vmem((PLANE, 8, genes), F32),
        vmem((lines, 8, genes), F32),
        vmem((8, genes), F32),
        vmem((2, rows, LANES), F32),
        vmem((3, rows, LANES), F32),
        vmem((PLANE, 8, rows), F32),
        vmem((spots, genes), BF16),
        vmem((spots, genes), BF16),
        vmem((spots, quarter), F32),
        vmem((PLANE, slide_rows, quarter), F32),
        vmem((PLANE, slide_rows, quarter), F32),
        vmem((PLANE, slide_rows, quarter), F32),
        vmem((PLANE, slide_rows, quarter), F32),
        vmem((slide_rows, cells), F32),
        vmem((slide_rows, cells), F32),
        vmem((cb, genes), F32),
        vmem((2, rows, LANES), F32),
        vmem((PLANE, 8, LANES), F32),
        vmem((lines, 8, LANES), F32),
        dma((2 * slides + 1,)),
        dma((chunks,)),
        dma((chunks,)),
        dma((chunks,)),
        dma((chunks,)),
        dma((chunks,)),
        dma((chunks,)),
        dma((chunks,)),
        dma((chunks,)),
        dma,
        dma((PLANE,)),
        dma,
        dma((PLANE,)),
        dma,
        dma((PLANE,)),
        dma((chunks,)),
        dma((chunks, PLANE)),
        dma,
        dma((2, PLANE)),
        dma,
        dma((2, lines)),
        dma,
        dma,
        dma((turns,)),
        dma((turns, PLANE)),
        dma((turns,)),
        dma((turns, lines)),
        dma((turns,)),
        dma((turns, lines)),
        dma,
        dma((PLANE,)),
        dma,
        dma,
        dma,
        dma,
        dma,
        dma,
        dma,
        dma((PLANE,)),
        dma,
        dma((lines,)),
        dma((slides + 3,)),
    ]
    for shape, widths in (
        ((quarter,), FORWARD),
        ((spots,), FORWARD),
        ((PLANE, rows), FORWARD),
        ((spots,), BACKWARD),
        ((quarter,), BACKWARD),
        ((quarter,), BACKWARD),
        ((quarter,), BACKWARD),
    ):
        scratch += [vmem(shape + (width,), F32) for width in widths]
    pred_shape = jax.ShapeDtypeStruct((slides, slide_rows, genes), F32)
    glog_shape = jax.ShapeDtypeStruct((slides, slide_rows, cells), F32)
    gexp_shape = jax.ShapeDtypeStruct((cb, genes), F32)
    pred, loss, grad_logits, grad_expr = pl.pallas_call(
        functools.partial(plane_kernel, lines, FORWARD, BACKWARD),
        out_shape=(pred_shape, jax.ShapeDtypeStruct((1, 1), F32), glog_shape, gexp_shape),
        in_specs=[anywhere, anywhere, anywhere, in_smem, in_vmem, in_vmem],
        out_specs=(anywhere, in_vmem, anywhere, anywhere),
        scratch_shapes=scratch,
        compiler_params=pltpu.CompilerParams(
            collective_id=0, has_side_effects=True, vmem_limit_bytes=56 * 1024 * 1024
        ),
    )(logits, expr, spatial, slide_spots, spot_cells, cell_prior.reshape(1, cells))
    pred, grad_logits, grad_expr = pl.pallas_call(
        deliver,
        out_shape=(pred_shape, glog_shape, gexp_shape),
        in_specs=[anywhere] * 3,
        out_specs=(anywhere,) * 3,
        scratch_shapes=[vmem(shape.shape, F32) for shape in (pred_shape, glog_shape, gexp_shape)] + [dma((2, 3))],
        compiler_params=pltpu.CompilerParams(vmem_limit_bytes=56 * 1024 * 1024),
    )(pred, grad_logits, grad_expr)
    return pred, loss.reshape(()), grad_logits, grad_expr


def general_plan(logits, expr, spatial, slide_spots, spot_cells, cell_prior):
    place = lax.axis_index("spot")
    side = lax.axis_index("gene")
    rows_all = logits.shape[1]
    cell_rows = expr.shape[0]
    weights = cell_prior.astype(jnp.float32) / fixed_point
    gene_share = (place == 0).astype(jnp.float32)
    row_share = (side == 0).astype(jnp.float32)
    own_weights = lax.dynamic_slice_in_dim(weights, place * cell_rows, cell_rows, 0)
    expr_acc = jnp.zeros((cell_rows, expr.shape[1]), jnp.float32)
    loss_local = jnp.zeros((), jnp.float32)
    pred_list = []
    grad_list = []
    for slide in range(logits.shape[0]):
        logit_rows = logits[slide]
        counted = spot_cells[slide].astype(jnp.float32)
        target = spatial[slide]
        positions = place * rows_all + jnp.arange(rows_all, dtype=jnp.int32)
        valid = (positions < slide_spots[slide]).astype(jnp.float32)
        peak = jnp.max(logit_rows, axis=1, keepdims=True)
        raised = jnp.exp(logit_rows - peak)
        probs = raised / jnp.sum(raised, axis=1, keepdims=True)
        mass = jnp.dot(probs, weights, precision=lax.Precision.HIGHEST)
        blocks = lax.all_to_all(probs, "spot", split_axis=1, concat_axis=0, tiled=True)
        pred = lax.psum_scatter(
            jnp.dot(blocks, expr, precision=lax.Precision.HIGHEST),
            "spot",
            scatter_dimension=0,
            tiled=True,
        )
        gene_dot = jnp.sum(valid[:, None] * pred * target, axis=0)
        gene_pred = jnp.sum(valid[:, None] * pred * pred, axis=0)
        gene_true = jnp.sum(valid[:, None] * target * target, axis=0)
        mass_part = jnp.sum(valid * mass)
        kcell = valid * counted
        cell_part = jnp.sum(kcell)
        spot_dot = jnp.sum(pred * target, axis=1)
        spot_pred = jnp.sum(pred * pred, axis=1)
        spot_true = jnp.sum(target * target, axis=1)
        gene_dot, gene_pred, gene_true, mass_total, cell_total = lax.psum(
            (gene_dot, gene_pred, gene_true, mass_part, cell_part), "spot"
        )
        spot_dot, spot_pred, spot_true = lax.psum((spot_dot, spot_pred, spot_true), "gene")
        gene_inv = lax.rsqrt(gene_pred * gene_true + tiny)
        cos_gene = gene_dot * gene_inv
        spot_inv = lax.rsqrt(spot_pred * spot_true + tiny)
        cos_spot = spot_dot * spot_inv
        share = kcell / cell_total
        scale_count = slide_spots[slide].astype(jnp.float32)
        kl_part = jnp.sum(
            share * (jnp.log(counted) - jnp.log(cell_total) - jnp.log(mass) + jnp.log(mass_total))
        )
        loss_local = loss_local - gene_share * jnp.sum(cos_gene)
        loss_local = loss_local + row_share * (scale_count * kl_part - jnp.sum(valid * cos_spot))
        gene_back = cos_gene * gene_true / (gene_pred * gene_true + tiny)
        spot_back = cos_spot * spot_true / (spot_pred * spot_true + tiny)
        dpred = -valid[:, None] * (
            target * (gene_inv[None, :] + spot_inv[:, None])
            - pred * gene_back[None, :]
            - pred * spot_back[:, None]
        )
        dmass = scale_count * valid * (1.0 / mass_total - share / mass)
        pred_list.append(pred)
        grads_full, mass_full = (
            lax.all_gather(dpred, "spot", axis=0, tiled=True),
            lax.all_gather(dmass, "spot", axis=0, tiled=True),
        )
        dprob_cells = jnp.dot(grads_full, expr.T, precision=lax.Precision.HIGHEST)
        dprob_cells = lax.psum(dprob_cells, "gene")
        expr_acc = expr_acc + lax.dot_general(
            blocks, grads_full, (((0,), (0,)), ((), ())), precision=lax.Precision.HIGHEST
        )
        dprob_cells = dprob_cells + mass_full[:, None] * own_weights[None, :]
        dprob_rows = lax.all_to_all(dprob_cells, "spot", split_axis=0, concat_axis=1, tiled=True)
        inner = jnp.sum(probs * dprob_rows, axis=1, keepdims=True)
        dlogit = probs * (dprob_rows - inner)
        grad_list.append(dlogit)
    loss = lax.psum(loss_local, ("spot", "gene"))
    return (jnp.stack(pred_list), loss, jnp.stack(grad_list), expr_acc)


def solution(mesh):
    places = mesh.shape["spot"]

    def on_device(logits, expr, spatial, slide_spots, spot_cells, cell_prior):
        if places == PLANE * PLANE and mesh.shape["gene"] == 2 and expr.shape[1] == sum(FORWARD):
            return plane_call(
                logits, expr, spatial, slide_spots, spot_cells, cell_prior, places // PLANE
            )
        return general_plan(logits, expr, spatial, slide_spots, spot_cells, cell_prior)

    in_specs = (
        P(None, "spot", None),
        P("spot", "gene"),
        P(None, "spot", "gene"),
        P(),
        P(None, "spot"),
        P(),
    )
    out_specs = (P(None, "spot", "gene"), P(), P(None, "spot", None), P("spot", "gene"))
    return jax.shard_map(
        on_device, mesh=mesh, in_specs=in_specs, out_specs=out_specs, check_vma=False
    )
```

```python
import functools

import jax
import jax.numpy as jnp
from jax import lax
from jax.experimental import pallas as pl
from jax.experimental.pallas import tpu as pltpu
from jax.sharding import PartitionSpec as P

tiny = 1e-06
fixed_point = 16384.0
F32 = jnp.float32
BF16 = jnp.bfloat16
MESH = pl.DeviceIdType.MESH

PLANE = 4
LANES = 128
STEP_ROWS = 16
FORWARD = (128, 256, 256, 256, 128)
BACKWARD = (128, 256, 256, 256, 128)
SPLIT = 2
LEAD = 2
FORWARD_STEPS = (
    ("far", 0),
    ("share",),
    ("near", 0),
    ("far", 1),
    ("near", 1),
    ("far", 2),
    ("far", 3),
    ("near", 2),
    ("take",),
    ("whole", 0),
    ("product", 0),
    ("whole", 1),
    ("product", 1),
    ("near", 3),
    ("far", 4),
    ("sum", 0),
    ("near", 4),
    ("whole", 2),
    ("product", 2),
    ("sum", 1),
    ("whole", 3),
    ("product", 3),
    ("turn", 0),
    ("turn", 1),
    ("whole", 4),
    ("product", 4),
    ("sum", 2),
    ("plane", 0),
    ("sum", 3),
    ("sum", 4),
    ("plane", 1),
    ("cores",),
    ("line", 0),
    ("line", 1),
)
EARLY = 3
BACKWARD_STEPS = (
    ("grad", 0),
    ("grad", 1),
    ("grad", 2),
    ("grad", 3),
    ("grad", 4),
    ("terms",),
    ("product", 0),
    ("product", 1),
    ("probs", 0, 384),
    ("add", 0),
    ("product", 2),
    ("product", 3),
    ("product", 4),
    ("probs", 384, 1024),
    ("cores",),
    ("add", 1),
    ("add", 2),
    ("return",),
    ("add", 3),
    ("loss",),
    ("expr", 0),
    ("logits",),
    ("add", 4),
    ("expr", 1),
    ("expr", 2),
    ("expr", 3),
    ("expr", 4),
)


def halves(value):
    high = value.astype(BF16)
    return high, (value - high.astype(F32)).astype(BF16)


def product(a_high, a_low, b_high, b_low, contract):
    def one(a, b):
        return lax.dot_general(a, b, (contract, ((), ())), preferred_element_type=F32)

    return one(a_high, b_high) + (one(a_high, b_low) + one(a_low, b_high))


def plane_kernel(lines, forward_widths, backward_widths, *refs):
    chunks, turns = len(forward_widths), len(backward_widths)
    (
        (logits_ref, expr_ref, spatial_ref, count_ref, cells_ref, prior_ref),
        (pred_ref, loss_ref, glog_ref, gexp_ref),
        (lg, lq, tg, ex, pq, ab, af, ahi, alo, thi, tlo, bhi, blo, pr, sacc, s1, s2, gv, ss, rowv, rs),
        (dhi, dlo, fs, fx, fy, fz, fr, go, gs, ge, inn, l1, l2),
        (loc, ou_s, ou_r, od_s, od_r, fu_s, fu_r, fd_s, fd_r, a_s, a_r, a2_s, a2_r, r_s, r_r),
        (c_s, c_r, s1_s, s1_r, s2_s, s2_r, ss_s, ss_r, d_s, d_r, ru_s, ru_r, rd_s, rd_r),
        (f_s, f_r, fx_s, fx_r, go_s, go_r, in_s, in_r, l1_s, l1_r, l2_s, l2_r, out_s),
        bb,
        cs,
        cr,
        ds,
        es,
        ru,
        rd,
    ) = grouped(refs, (6, 4, 21, 13, 15, 14, 13, chunks, chunks, chunks, turns, turns, turns, turns))
    place = lax.axis_index("spot")
    core = lax.axis_index("gene")
    z = place // PLANE
    q = place % PLANE
    col, row = q % 2, q // 2
    mates = ((1 - row) * 2 + 1 - col, row * 2 + 1 - col, (1 - row) * 2 + col)
    others = tuple((z + step) % lines for step in range(1, lines))
    up, down = (place + PLANE, core), (place - PLANE, core)
    sibling = (place, 1 - core)
    slides, slide_rows = logits_ref.shape[0], logits_ref.shape[1]
    rows = slides * slide_rows
    cb = expr_ref.shape[0]
    genes = expr_ref.shape[1]
    last = lines - 1

    def mate(p):
        return (z * PLANE + p, core)

    def send(src, dst, send_sem, recv_sem, device):
        copy = pltpu.make_async_remote_copy(
            src_ref=src, dst_ref=dst, send_sem=send_sem, recv_sem=recv_sem, device_id=device, device_id_type=MESH
        )
        copy.start()

    def arrived(dst, recv_sem):
        pltpu.make_async_copy(dst, dst, recv_sem).wait()

    sent = arrived

    def cols(k):
        return pl.ds(sum(forward_widths[:k]), forward_widths[k])

    def turn_cols(k):
        return pl.ds(sum(backward_widths[:k]), backward_widths[k])

    def block(index):
        return pl.ds(pl.multiple_of(index * cb, cb), cb)

    def share(index):
        return pl.ds(pl.multiple_of(index * rows, rows), rows)

    def half(index):
        return pl.ds(pl.multiple_of(index * slide_rows, slide_rows), slide_rows)

    for m in range(slides):
        pltpu.make_async_copy(logits_ref.at[m], lg.at[half(m)], loc.at[m]).start()
        pltpu.make_async_copy(spatial_ref.at[m], tg.at[half(m)], loc.at[slides + m]).start()
    pltpu.make_async_copy(expr_ref, ex, loc.at[2 * slides]).start()

    barrier = pltpu.get_barrier_semaphore()
    for p in mates:
        pl.semaphore_signal(barrier, inc=1, device_id=mate(p), device_id_type=MESH)
    for o in others:
        pl.semaphore_signal(barrier, inc=1, device_id=(o * PLANE + q, core), device_id_type=MESH)
    pl.semaphore_signal(barrier, inc=1, device_id=sibling, device_id_type=MESH)
    pl.semaphore_wait(barrier, len(mates) + len(others) + 1)

    for m in range(slides):
        pltpu.make_async_copy(logits_ref.at[m], lg.at[half(m)], loc.at[m]).wait()
    for p in range(PLANE):
        for line in range(lines):
            lq[p, :, pl.ds(line * cb, cb)] = lg[half(core), pl.ds((line * PLANE + p) * cb, cb)]
    for p in mates:
        send(lq.at[p], ab.at[q, half(core)], a_s, a_r.at[q], mate(p))

    pltpu.make_async_copy(expr_ref, ex, loc.at[2 * slides]).wait()
    for k in range(chunks):
        bb[k][block(z), :] = ex[:, cols(k)]

    def own_up(k):
        here = bb[k].at[block(z)]
        send(here, here, ou_s.at[k], ou_r.at[k], up)

    def own_down(k):
        here = bb[k].at[block(z)]
        send(here, here, od_s.at[k], od_r.at[k], down)

    def low(at):
        return 2 * at < lines

    for at in range(lines):

        @pl.when(z == at)
        def _():
            for k in range(chunks):
                if at < last and (not low(at) or at == 0 or k < LEAD):
                    own_up(k)
                if at > 0 and (low(at) or at == last or k < LEAD):
                    own_down(k)

    def from_below(k, at):
        arrived(bb[k].at[pl.ds((at - 1) * cb, cb)], ou_r.at[k])
        if at > 1:
            arrived(bb[k].at[pl.ds(0, (at - 1) * cb)], fu_r.at[k])

    def from_above(k, at):
        arrived(bb[k].at[pl.ds((at + 1) * cb, cb)], od_r.at[k])
        if at < last - 1:
            arrived(bb[k].at[pl.ds((at + 2) * cb, (last - 1 - at) * cb)], fd_r.at[k])

    def upward(k, at):
        from_below(k, at)
        here = bb[k].at[pl.ds(0, at * cb)]
        send(here, here, fu_s.at[k], fu_r.at[k], up)

    def downward(k, at):
        from_above(k, at)
        here = bb[k].at[pl.ds((at + 1) * cb, (last - at) * cb)]
        send(here, here, fd_s.at[k], fd_r.at[k], down)

    def forward_far(k):
        for at in range(1, last):

            @pl.when(z == at)
            def _():
                (upward if low(at) else downward)(k, at)
                if k + LEAD < chunks:
                    (own_up if low(at) else own_down)(k + LEAD)

    def forward_near(k):
        for at in range(1, last):

            @pl.when(z == at)
            def _():
                (downward if low(at) else upward)(k, at)

    def gathered(k):
        @pl.when(z == 0)
        def _():
            from_above(k, 0)

        @pl.when(z == last)
        def _():
            from_below(k, last)

    weights = prior_ref[...].astype(F32) / fixed_point

    @pl.loop(0, rows // STEP_ROWS)
    def _(step):
        at = pl.ds(pl.multiple_of(step * STEP_ROWS, STEP_ROWS), STEP_ROWS)
        value = lg[at, :]
        peak = jnp.max(value, axis=1, keepdims=True)
        raised = jnp.exp(value - peak)
        scale = 1.0 / jnp.sum(raised, axis=1, keepdims=True)
        probs = raised * scale
        mass_rows = jnp.sum(probs * weights, axis=1, keepdims=True)
        rowv[0, at, :] = jnp.broadcast_to(mass_rows, (STEP_ROWS, LANES))
        rowv[1, at, :] = jnp.broadcast_to(peak, (STEP_ROWS, LANES))
        rowv[2, at, :] = jnp.broadcast_to(scale, (STEP_ROWS, LANES))
        for p in range(PLANE):
            for line in range(lines):
                at_cells = (line * PLANE + p) * cb
                pq[p, at, pl.ds(line * cb, cb)] = probs[:, at_cells : at_cells + cb]

    wide = lax.broadcasted_iota(jnp.int32, (rows, LANES), 1)
    rs[q] = jnp.where(wide == 0, rowv[1], rowv[2]).T[0:8]
    for p in mates:
        send(rs.at[q], rs.at[q], r_s, r_r.at[q], mate(p))

    rid = lax.broadcasted_iota(jnp.int32, (rows, 1), 0)
    first = rid < slide_rows
    position = place * slide_rows + jnp.where(first, rid, rid - slide_rows)
    count = jnp.where(first, count_ref[0], count_ref[1])
    valid = (position < count).astype(F32)
    scale_count = count.astype(F32)
    square = (slide_rows, slide_rows)
    eye = lax.broadcasted_iota(jnp.int32, square, 0) == lax.broadcasted_iota(jnp.int32, square, 1)
    counted = jnp.concatenate(
        [
            jnp.sum(jnp.where(eye, cells_ref[m : m + 1, :].astype(F32), 0.0), axis=1, keepdims=True)
            for m in range(slides)
        ],
        axis=0,
    )
    mass = rowv[0, :, 0:1]
    kcell = valid * counted

    def by_slide(value):
        return [jnp.sum(value[m * slide_rows : (m + 1) * slide_rows], axis=0, keepdims=True) for m in range(slides)]

    mass_parts = by_slide(valid * mass)
    cell_parts = by_slide(kcell)
    lane = lax.broadcasted_iota(jnp.int32, (1, LANES), 1)
    scalars = jnp.zeros((1, LANES), F32)
    for at, value in enumerate(mass_parts + cell_parts):
        scalars = jnp.where(lane == at, value, scalars)
    for m in range(slides):
        pltpu.make_async_copy(spatial_ref.at[m], tg.at[half(m)], loc.at[slides + m]).wait()
    sacc[...] = jnp.zeros_like(sacc)
    s1[q, 3 * slides :, :] = jnp.zeros((8 - 3 * slides, genes), F32)
    s1[q, 3 * slides : 3 * slides + 1, 0:LANES] = scalars

    def share_logits():
        for p in (mates[1], mates[2], mates[0]):
            here = ab.at[p, half(core)]
            arrived(here, a_r.at[p])
            send(here, here, a2_s, a2_r.at[p], sibling)

    def take_probs():
        af[q] = pq[q]
        ahi[share(q), :], alo[share(q), :] = halves(pq[q])
        for p in (mates[1], mates[2], mates[0]):
            arrived(rs.at[p], r_r.at[p])
            arrived(ab.at[p, half(1 - core)], a2_r.at[p])
            by_row = rs[p].T
            probs = jnp.exp(ab[p] - by_row[:, 0:1]) * by_row[:, 1:2]
            af[p] = probs
            ahi[share(p), :], alo[share(p), :] = halves(probs)

    def transpose(part):
        for p in (2 * part, 2 * part + 1):
            high, low_part = halves(af[p].T)
            thi[:, share(p)], tlo[:, share(p)] = high, low_part

    def forward_product(k):
        high, low = halves(bb[k][...])
        bhi[:, cols(k)], blo[:, cols(k)] = high, low
        cs[k][...] = product(ahi[...], alo[...], high, low, ((1,), (0,)))
        for p in mates:
            send(cs[k].at[share(p)], cr[k].at[q], c_s.at[k], c_r.at[k, q], mate(p))

    def finish_pred(k):
        total = cs[k][share(q), :]
        for p in mates:
            arrived(cr[k].at[p], c_r.at[k, p])
            total = total + cr[k][p]
        pr[:, cols(k)] = total
        truth = tg[:, cols(k)]
        for at, value in enumerate((total * truth, total * total, truth * truth)):
            sacc[at] += lane_groups(value)
        kept = valid * total
        stats = by_slide(kept * truth) + by_slide(kept * total) + by_slide(valid * truth * truth)
        s1[q, 0 : 3 * slides, cols(k)] = jnp.concatenate(stats, axis=0)

    early = sum(forward_widths[:EARLY])
    parts = (pl.ds(0, early), pl.ds(early, genes - early))

    def sum_plane(at):
        for p in mates:
            send(s1.at[q, :, parts[at]], s1.at[q, :, parts[at]], s1_s, s1_r.at[at, q], mate(p))

    def sum_line(at):
        for p in mates:
            arrived(s1.at[p, :, parts[at]], s1_r.at[at, p])
        s2[z, :, parts[at]] = (s1[0, :, parts[at]] + s1[1, :, parts[at]]) + (s1[2, :, parts[at]] + s1[3, :, parts[at]])
        for o in others:
            send(s2.at[z, :, parts[at]], s2.at[z, :, parts[at]], s2_s, s2_r.at[at, z], (o * PLANE + q, core))

    def sum_cores():
        sums = [jnp.sum(sacc[at], axis=1, keepdims=True) for at in range(3)]
        ss[core] = jnp.where(wide == 0, sums[0], jnp.where(wide == 1, sums[1], sums[2]))
        send(ss.at[core], ss.at[core], ss_s, ss_r, sibling)

    steps = {
        "far": forward_far,
        "near": forward_near,
        "share": share_logits,
        "take": take_probs,
        "whole": gathered,
        "product": forward_product,
        "sum": finish_pred,
        "turn": transpose,
        "plane": sum_plane,
        "cores": sum_cores,
        "line": sum_line,
    }
    for name, *where in FORWARD_STEPS:
        steps[name](*where)

    for m in range(slides):
        pltpu.make_async_copy(pr.at[half(m)], pred_ref.at[m], out_s.at[m]).start()
    arrived(ss.at[1 - core], ss_r)
    spot = ss[0] + ss[1]
    spot_dot, spot_pred, spot_true = spot[:, 0:1], spot[:, 1:2], spot[:, 2:3]
    spot_inv = lax.rsqrt(spot_pred * spot_true + tiny)
    cos_spot = spot_dot * spot_inv
    spot_back = cos_spot * spot_true / (spot_pred * spot_true + tiny)
    for o in others:
        for at in range(2):
            arrived(s2.at[o, :, parts[at]], s2_r.at[at, o])
    total = s2[0]
    for line in range(1, lines):
        total = total + s2[line]
    gene_dot, gene_pred, gene_true = total[0:2], total[2:4], total[4:6]
    gene_inv = lax.rsqrt(gene_pred * gene_true + tiny)
    cos_gene = gene_dot * gene_inv
    gv[0:2, :] = gene_inv
    gv[2:4, :] = cos_gene * gene_true / (gene_pred * gene_true + tiny)

    sacc[0] = jnp.zeros_like(sacc[0])

    def send_grad(k):
        pieces = []
        for m in range(slides):
            lo, hi = m * slide_rows, (m + 1) * slide_rows
            truth, guess = tg[lo:hi, turn_cols(k)], pr[lo:hi, turn_cols(k)]
            inverse, back = gv[m : m + 1, turn_cols(k)], gv[2 + m : 3 + m, turn_cols(k)]
            pieces.append(
                -valid[lo:hi]
                * (truth * (inverse + spot_inv[lo:hi]) - guess * back - guess * spot_back[lo:hi])
            )
        grad = jnp.concatenate(pieces, axis=0)
        here = ds[k].at[share(q)]
        here[...] = grad
        for p in mates:
            send(here, here, d_s.at[k], d_r.at[k, q], mate(p))
        sacc[0] += lane_groups(grad * pr[:, turn_cols(k)])

    gene_sum = jnp.sum(jnp.sum(cos_gene, axis=1, keepdims=True), axis=0, keepdims=True)

    mass_total = jnp.where(first, total[6:7, 0:1], total[6:7, 1:2])
    cell_total = jnp.where(first, total[6:7, 2:3], total[6:7, 3:4])
    portion = kcell / cell_total
    kl_rows = portion * (jnp.log(counted) - jnp.log(cell_total) - jnp.log(mass) + jnp.log(mass_total))
    dmass = scale_count * valid * (1.0 / mass_total - portion / mass)
    terms = jnp.sum(scale_count * kl_rows - valid * cos_spot, axis=0, keepdims=True)

    def send_terms():
        l1[q] = jnp.broadcast_to(terms, (8, LANES))
        for p in mates:
            send(l1.at[q], l1.at[q], l1_s, l1_r.at[q], mate(p))
        inner = jnp.sum(sacc[0], axis=1, keepdims=True)
        inn[core] = jnp.where(wide == 0, inner, gene_sum)
        send(inn.at[core], inn.at[core], in_s, in_r, sibling)
        rowv[1] = jnp.broadcast_to(dmass, (rows, LANES))


    def backward_product(k):
        for p in mates:
            arrived(ds[k].at[share(p)], d_r.at[k, p])
        high, low = halves(ds[k][...])
        dhi[:, turn_cols(k)], dlo[:, turn_cols(k)] = high, low
        es[k][...] = product(thi[...], tlo[...], high, low, ((1,), (0,)))

        @pl.when(z == 0)
        def _():
            if whole(k):
                pass_up(k, 1, last)
            else:
                for line in range(last, 0, -1):
                    pass_up(k, line, 1)

        @pl.when(z == last)
        def _():
            if whole(k):
                pass_down(k, 0, last)
            else:
                for line in range(last):
                    pass_down(k, line, 1)

    def whole(k):
        return k < turns - SPLIT

    def pass_up(k, line, count):
        here = pl.ds(line * cb, count * cb)
        send(es[k].at[here], ru[k].at[here], ru_s.at[k], ru_r.at[k, 0 if whole(k) else line], up)

    def pass_down(k, line, count):
        here = pl.ds(line * cb, count * cb)
        send(es[k].at[here], rd[k].at[here], rd_s.at[k], rd_r.at[k, 0 if whole(k) else line], down)

    def take_up(k, line, count):
        here = pl.ds(line * cb, count * cb)
        arrived(ru[k].at[here], ru_r.at[k, 0 if whole(k) else line])

    def take_down(k, line, count):
        here = pl.ds(line * cb, count * cb)
        arrived(rd[k].at[here], rd_r.at[k, 0 if whole(k) else line])

    def add_on(k):
        for at in range(1, last):

            @pl.when(z == at)
            def _():
                def rising():
                    if whole(k):
                        take_up(k, at, lines - at)
                        above = pl.ds((at + 1) * cb, (last - at) * cb)
                        es[k][above, :] += ru[k][above, :]
                        pass_up(k, at + 1, last - at)
                    else:
                        for line in range(last, at, -1):
                            take_up(k, line, 1)
                            here = pl.ds(line * cb, cb)
                            es[k][here, :] += ru[k][here, :]
                            pass_up(k, line, 1)

                def falling():
                    if whole(k):
                        take_down(k, 0, at + 1)
                        below = pl.ds(0, at * cb)
                        es[k][below, :] += rd[k][below, :]
                        pass_down(k, 0, at)
                    else:
                        for line in range(at):
                            take_down(k, line, 1)
                            here = pl.ds(line * cb, cb)
                            es[k][here, :] += rd[k][here, :]
                            pass_down(k, line, 1)

                for step in (rising, falling) if low(at) else (falling, rising):
                    step()

    def finish_expr(k):
        for at in range(lines):

            @pl.when(z == at)
            def _():
                own = pl.ds(at * cb, cb)
                total = es[k][own, :]
                if at > 0:
                    if at == last or not whole(k):
                        take_up(k, at, 1)
                    total = total + ru[k][own, :]
                if at < last:
                    if at == 0 or not whole(k):
                        take_down(k, at, 1)
                    total = total + rd[k][own, :]
                ge[:, turn_cols(k)] = total

    def probs_gradient(start, end):
        at = pl.ds(start, end - start)
        part = product(dhi[:, at], dlo[:, at], bhi[:, at], blo[:, at], ((1,), (1,)))
        if start == 0:
            fs[...] = part
        else:
            fs[...] += part

    def slide_of(p, m):
        return pl.ds(pl.multiple_of(p * rows + m * slide_rows, slide_rows), slide_rows)

    def sum_probs_cores():
        for p in mates + (q,):
            fx[p] = fs[slide_of(p, 1 - core), :]
            send(fx.at[p], fy.at[p], fx_s, fx_r.at[p], sibling)

    def return_probs():
        for p in mates + (q,):
            arrived(fy.at[p], fx_r.at[p])
            fz[p] = fs[slide_of(p, core), :] + fy[p]
        for p in mates:
            send(fz.at[p], fr.at[q], f_s, f_r.at[q], mate(p))
        fr[q] = fz[q]

    def pass_terms():
        for p in mates:
            arrived(l1.at[p], l1_r.at[p])
        l2[z] = (l1[0] + l1[1]) + (l1[2] + l1[3])
        for o in others:
            send(l2.at[z], l2.at[z], l2_s, l2_r.at[z], (o * PLANE + q, core))

    def finish_logits():
        arrived(inn.at[1 - core], in_r)
        rowv[2] = (inn[0] + inn[1]) + rowv[1] * rowv[0]
        for p in mates:
            arrived(fr.at[p], f_r.at[p])
        for m in range(2):

            @pl.loop(0, slide_rows // STEP_ROWS // 2)
            def _(step):
                row_at = (m * (slide_rows // STEP_ROWS // 2) + step) * STEP_ROWS
                at = pl.ds(pl.multiple_of(row_at, STEP_ROWS), STEP_ROWS)
                whole_at = pl.ds(pl.multiple_of(core * slide_rows + row_at, STEP_ROWS), STEP_ROWS)
                by_mass, total_inner = rowv[1, whole_at, 0:1], rowv[2, whole_at, 0:1]
                for p in range(PLANE):
                    for line in range(lines):
                        here, there = pl.ds(line * cb, cb), (line * PLANE + p) * cb
                        grad = fr[p, at, here] + by_mass * weights[:, there : there + cb]
                        go[at, pl.ds(there, cb)] = pq[p, whole_at, here] * (grad - total_inner)

            part = pl.ds(m * (slide_rows // 2), slide_rows // 2)
            send(go.at[part], gs.at[part], go_s, go_r.at[m], sibling)
        pltpu.make_async_copy(go, glog_ref.at[core], out_s.at[slides + 1]).start()

    steps = {
        "grad": send_grad,
        "terms": send_terms,
        "product": backward_product,
        "probs": probs_gradient,
        "cores": sum_probs_cores,
        "return": return_probs,
        "loss": pass_terms,
        "logits": finish_logits,
        "add": add_on,
        "expr": finish_expr,
    }
    for name, *where in BACKWARD_STEPS:
        steps[name](*where)
    pltpu.make_async_copy(ge, gexp_ref, out_s.at[slides]).start()

    for o in others:
        arrived(l2.at[o], l2_r.at[o])
    loss = l2[0]
    for line in range(1, lines):
        loss = loss + l2[line]
    loss_ref[...] = loss[0:1, 0:1] - (inn[0, 0:1, 1:2] + inn[1, 0:1, 1:2])
    for m in range(2):
        arrived(gs.at[pl.ds(m * (slide_rows // 2), slide_rows // 2)], go_r.at[m])
    pltpu.make_async_copy(gs, glog_ref.at[1 - core], out_s.at[slides + 2]).start()

    for m in range(slides):
        pltpu.make_async_copy(pr.at[half(m)], pred_ref.at[m], out_s.at[m]).wait()
    pltpu.make_async_copy(ge, gexp_ref, out_s.at[slides]).wait()
    pltpu.make_async_copy(go, glog_ref.at[core], out_s.at[slides + 1]).wait()
    pltpu.make_async_copy(gs, glog_ref.at[1 - core], out_s.at[slides + 2]).wait()
    for k in range(chunks):

        @pl.when(z < last)
        def _():
            sent(bb[k].at[block(z)], ou_s.at[k])

        @pl.when(z > 0)
        def _():
            sent(bb[k].at[block(z)], od_s.at[k])

        for at in range(1, last):

            @pl.when(z == at)
            def _():
                sent(bb[k].at[pl.ds(0, at * cb)], fu_s.at[k])
                sent(bb[k].at[pl.ds((at + 1) * cb, (last - at) * cb)], fd_s.at[k])

    for k in range(turns):
        for at in range(lines):

            @pl.when(z == at)
            def _():
                if at < last:
                    sent(es[k].at[pl.ds((at + 1) * cb, (last - at) * cb)], ru_s.at[k])
                if at > 0:
                    sent(es[k].at[pl.ds(0, at * cb)], rd_s.at[k])

    three = pl.ds(0, len(mates))
    sent(ab.at[three, half(0)], a_s)
    sent(ab.at[three, half(0)], a2_s)
    sent(rs.at[three], r_s)
    for k in range(chunks):
        sent(cr[k].at[three], c_s.at[k])
    sent(s1.at[three], s1_s)
    sent(s2.at[pl.ds(0, last)], s2_s)
    sent(ss.at[0], ss_s)
    for k in range(turns):
        sent(ds[k].at[pl.ds(0, len(mates) * rows)], d_s.at[k])
    sent(inn.at[0], in_s)
    sent(l1.at[three], l1_s)
    sent(l2.at[pl.ds(0, last)], l2_s)
    sent(fr.at[three], f_s)
    sent(fx, fx_s)
    sent(go, go_s)


def lane_groups(value):
    parts = [value[:, at : at + LANES] for at in range(0, value.shape[1], LANES)]
    return functools.reduce(lambda a, b: a + b, parts)


def grouped(refs, sizes):
    at = 0
    for size in sizes:
        yield refs[at : at + size]
        at += size


def deliver(pred_in, glog_in, gexp_in, pred_ref, glog_ref, gexp_ref, pred_mid, glog_mid, gexp_mid, sems):
    triples = ((glog_in, glog_mid, glog_ref), (pred_in, pred_mid, pred_ref), (gexp_in, gexp_mid, gexp_ref))
    loads = [pltpu.make_async_copy(src, mid, sems.at[0, at]) for at, (src, mid, _) in enumerate(triples)]
    stores = [pltpu.make_async_copy(mid, dst, sems.at[1, at]) for at, (_, mid, dst) in enumerate(triples)]
    for load in loads:
        load.start()
    for load, store in zip(loads, stores):
        load.wait()
        store.start()
    for store in stores:
        store.wait()


def plane_call(logits, expr, spatial, slide_spots, spot_cells, cell_prior, lines):
    slides, slide_rows, cells = logits.shape
    rows = slides * slide_rows
    cb, genes = expr.shape
    quarter = lines * cb
    spots = PLANE * rows
    chunks, turns = len(FORWARD), len(BACKWARD)
    dma = pltpu.SemaphoreType.DMA
    vmem = pltpu.VMEM
    anywhere = pl.BlockSpec(memory_space=pl.ANY)
    in_vmem = pl.BlockSpec(memory_space=pltpu.VMEM)
    in_smem = pl.BlockSpec(memory_space=pltpu.SMEM)
    scratch = [
        vmem((rows, cells), F32),
        vmem((PLANE, slide_rows, quarter), F32),
        vmem((rows, genes), F32),
        vmem((cb, genes), F32),
        vmem((PLANE, rows, quarter), F32),
        vmem((PLANE, rows, quarter), F32),
        vmem((PLANE, rows, quarter), F32),
        vmem((spots, quarter), BF16),
        vmem((spots, quarter), BF16),
        vmem((quarter, spots), BF16),
        vmem((quarter, spots), BF16),
        vmem((quarter, genes), BF16),
        vmem((quarter, genes), BF16),
        vmem((rows, genes), F32),
        vmem((3, rows, LANES), F32),
        vmem((PLANE, 8, genes), F32),
        vmem((lines, 8, genes), F32),
        vmem((8, genes), F32),
        vmem((2, rows, LANES), F32),
        vmem((3, rows, LANES), F32),
        vmem((PLANE, 8, rows), F32),
        vmem((spots, genes), BF16),
        vmem((spots, genes), BF16),
        vmem((spots, quarter), F32),
        vmem((PLANE, slide_rows, quarter), F32),
        vmem((PLANE, slide_rows, quarter), F32),
        vmem((PLANE, slide_rows, quarter), F32),
        vmem((PLANE, slide_rows, quarter), F32),
        vmem((slide_rows, cells), F32),
        vmem((slide_rows, cells), F32),
        vmem((cb, genes), F32),
        vmem((2, rows, LANES), F32),
        vmem((PLANE, 8, LANES), F32),
        vmem((lines, 8, LANES), F32),
        dma((2 * slides + 1,)),
        dma((chunks,)),
        dma((chunks,)),
        dma((chunks,)),
        dma((chunks,)),
        dma((chunks,)),
        dma((chunks,)),
        dma((chunks,)),
        dma((chunks,)),
        dma,
        dma((PLANE,)),
        dma,
        dma((PLANE,)),
        dma,
        dma((PLANE,)),
        dma((chunks,)),
        dma((chunks, PLANE)),
        dma,
        dma((2, PLANE)),
        dma,
        dma((2, lines)),
        dma,
        dma,
        dma((turns,)),
        dma((turns, PLANE)),
        dma((turns,)),
        dma((turns, lines)),
        dma((turns,)),
        dma((turns, lines)),
        dma,
        dma((PLANE,)),
        dma,
        dma((PLANE,)),
        dma,
        dma((2,)),
        dma,
        dma,
        dma,
        dma((PLANE,)),
        dma,
        dma((lines,)),
        dma((slides + 3,)),
    ]
    for shape, widths in (
        ((quarter,), FORWARD),
        ((spots,), FORWARD),
        ((PLANE, rows), FORWARD),
        ((spots,), BACKWARD),
        ((quarter,), BACKWARD),
        ((quarter,), BACKWARD),
        ((quarter,), BACKWARD),
    ):
        scratch += [vmem(shape + (width,), F32) for width in widths]
    pred_shape = jax.ShapeDtypeStruct((slides, slide_rows, genes), F32)
    glog_shape = jax.ShapeDtypeStruct((slides, slide_rows, cells), F32)
    gexp_shape = jax.ShapeDtypeStruct((cb, genes), F32)
    pred, loss, grad_logits, grad_expr = pl.pallas_call(
        functools.partial(plane_kernel, lines, FORWARD, BACKWARD),
        out_shape=(pred_shape, jax.ShapeDtypeStruct((1, 1), F32), glog_shape, gexp_shape),
        in_specs=[anywhere, anywhere, anywhere, in_smem, in_vmem, in_vmem],
        out_specs=(anywhere, in_vmem, anywhere, anywhere),
        scratch_shapes=scratch,
        compiler_params=pltpu.CompilerParams(
            collective_id=0, has_side_effects=True, vmem_limit_bytes=56 * 1024 * 1024
        ),
    )(logits, expr, spatial, slide_spots, spot_cells, cell_prior.reshape(1, cells))
    pred, grad_logits, grad_expr = pl.pallas_call(
        deliver,
        out_shape=(pred_shape, glog_shape, gexp_shape),
        in_specs=[anywhere] * 3,
        out_specs=(anywhere,) * 3,
        scratch_shapes=[vmem(shape.shape, F32) for shape in (pred_shape, glog_shape, gexp_shape)] + [dma((2, 3))],
        compiler_params=pltpu.CompilerParams(vmem_limit_bytes=56 * 1024 * 1024),
    )(pred, grad_logits, grad_expr)
    return pred, loss.reshape(()), grad_logits, grad_expr


def general_plan(logits, expr, spatial, slide_spots, spot_cells, cell_prior):
    place = lax.axis_index("spot")
    side = lax.axis_index("gene")
    rows_all = logits.shape[1]
    cell_rows = expr.shape[0]
    weights = cell_prior.astype(jnp.float32) / fixed_point
    gene_share = (place == 0).astype(jnp.float32)
    row_share = (side == 0).astype(jnp.float32)
    own_weights = lax.dynamic_slice_in_dim(weights, place * cell_rows, cell_rows, 0)
    expr_acc = jnp.zeros((cell_rows, expr.shape[1]), jnp.float32)
    loss_local = jnp.zeros((), jnp.float32)
    pred_list = []
    grad_list = []
    for slide in range(logits.shape[0]):
        logit_rows = logits[slide]
        counted = spot_cells[slide].astype(jnp.float32)
        target = spatial[slide]
        positions = place * rows_all + jnp.arange(rows_all, dtype=jnp.int32)
        valid = (positions < slide_spots[slide]).astype(jnp.float32)
        peak = jnp.max(logit_rows, axis=1, keepdims=True)
        raised = jnp.exp(logit_rows - peak)
        probs = raised / jnp.sum(raised, axis=1, keepdims=True)
        mass = jnp.dot(probs, weights, precision=lax.Precision.HIGHEST)
        blocks = lax.all_to_all(probs, "spot", split_axis=1, concat_axis=0, tiled=True)
        pred = lax.psum_scatter(
            jnp.dot(blocks, expr, precision=lax.Precision.HIGHEST),
            "spot",
            scatter_dimension=0,
            tiled=True,
        )
        gene_dot = jnp.sum(valid[:, None] * pred * target, axis=0)
        gene_pred = jnp.sum(valid[:, None] * pred * pred, axis=0)
        gene_true = jnp.sum(valid[:, None] * target * target, axis=0)
        mass_part = jnp.sum(valid * mass)
        kcell = valid * counted
        cell_part = jnp.sum(kcell)
        spot_dot = jnp.sum(pred * target, axis=1)
        spot_pred = jnp.sum(pred * pred, axis=1)
        spot_true = jnp.sum(target * target, axis=1)
        gene_dot, gene_pred, gene_true, mass_total, cell_total = lax.psum(
            (gene_dot, gene_pred, gene_true, mass_part, cell_part), "spot"
        )
        spot_dot, spot_pred, spot_true = lax.psum((spot_dot, spot_pred, spot_true), "gene")
        gene_inv = lax.rsqrt(gene_pred * gene_true + tiny)
        cos_gene = gene_dot * gene_inv
        spot_inv = lax.rsqrt(spot_pred * spot_true + tiny)
        cos_spot = spot_dot * spot_inv
        share = kcell / cell_total
        scale_count = slide_spots[slide].astype(jnp.float32)
        kl_part = jnp.sum(
            share * (jnp.log(counted) - jnp.log(cell_total) - jnp.log(mass) + jnp.log(mass_total))
        )
        loss_local = loss_local - gene_share * jnp.sum(cos_gene)
        loss_local = loss_local + row_share * (scale_count * kl_part - jnp.sum(valid * cos_spot))
        gene_back = cos_gene * gene_true / (gene_pred * gene_true + tiny)
        spot_back = cos_spot * spot_true / (spot_pred * spot_true + tiny)
        dpred = -valid[:, None] * (
            target * (gene_inv[None, :] + spot_inv[:, None])
            - pred * gene_back[None, :]
            - pred * spot_back[:, None]
        )
        dmass = scale_count * valid * (1.0 / mass_total - share / mass)
        pred_list.append(pred)
        grads_full, mass_full = (
            lax.all_gather(dpred, "spot", axis=0, tiled=True),
            lax.all_gather(dmass, "spot", axis=0, tiled=True),
        )
        dprob_cells = jnp.dot(grads_full, expr.T, precision=lax.Precision.HIGHEST)
        dprob_cells = lax.psum(dprob_cells, "gene")
        expr_acc = expr_acc + lax.dot_general(
            blocks, grads_full, (((0,), (0,)), ((), ())), precision=lax.Precision.HIGHEST
        )
        dprob_cells = dprob_cells + mass_full[:, None] * own_weights[None, :]
        dprob_rows = lax.all_to_all(dprob_cells, "spot", split_axis=0, concat_axis=1, tiled=True)
        inner = jnp.sum(probs * dprob_rows, axis=1, keepdims=True)
        dlogit = probs * (dprob_rows - inner)
        grad_list.append(dlogit)
    loss = lax.psum(loss_local, ("spot", "gene"))
    return (jnp.stack(pred_list), loss, jnp.stack(grad_list), expr_acc)


def solution(mesh):
    places = mesh.shape["spot"]

    def on_device(logits, expr, spatial, slide_spots, spot_cells, cell_prior):
        if places == PLANE * PLANE and mesh.shape["gene"] == 2 and expr.shape[1] == sum(FORWARD):
            return plane_call(
                logits, expr, spatial, slide_spots, spot_cells, cell_prior, places // PLANE
            )
        return general_plan(logits, expr, spatial, slide_spots, spot_cells, cell_prior)

    in_specs = (
        P(None, "spot", None),
        P("spot", "gene"),
        P(None, "spot", "gene"),
        P(),
        P(None, "spot"),
        P(),
    )
    out_specs = (P(None, "spot", "gene"), P(), P(None, "spot", None), P("spot", "gene"))
    return jax.shard_map(
        on_device, mesh=mesh, in_specs=in_specs, out_specs=out_specs, check_vma=False
    )
```

```python
import functools

import jax
import jax.numpy as jnp
from jax import lax
from jax.experimental import pallas as pl
from jax.experimental.pallas import tpu as pltpu
from jax.sharding import PartitionSpec as P

tiny = 1e-06
fixed_point = 16384.0
F32 = jnp.float32
BF16 = jnp.bfloat16
MESH = pl.DeviceIdType.MESH

PLANE = 4
LANES = 128
STEP_ROWS = 16
FORWARD = (256, 256, 256, 128, 128)
BACKWARD = (128, 256, 256, 256, 128)
SPLIT = 3
LEAD = 2
FORWARD_STEPS = (
    ("far", 0),
    ("share",),
    ("far", 1),
    ("near", 0),
    ("far", 2),
    ("near", 1),
    ("take",),
    ("turn", 0),
    ("whole", 0),
    ("product", 0),
    ("far", 3),
    ("near", 2),
    ("turn", 1),
    ("whole", 1),
    ("product", 1),
    ("whole", 2),
    ("near", 3),
    ("far", 4),
    ("product", 2),
    ("whole", 3),
    ("product", 3),
    ("whole", 4),
    ("near", 4),
    ("product", 4),
    ("sum", 0),
    ("sum", 1),
    ("sum", 2),
    ("plane", 0),
    ("sum", 3),
    ("sum", 4),
    ("plane", 1),
    ("cores",),
    ("line", 0),
    ("line", 1),
)
EARLY = 3
BACKWARD_STEPS = (
    ("grad", 0),
    ("grad", 1),
    ("grad", 2),
    ("grad", 3),
    ("grad", 4),
    ("terms",),
    ("product", 0),
    ("product", 1),
    ("probs", 0),
    ("product", 2),
    ("add_near", 0),
    ("probs", 1),
    ("probs", 2),
    ("product", 3),
    ("add_near", 1),
    ("probs", 3),
    ("product", 4),
    ("probs", 4),
    ("cores",),
    ("add_near", 2),
    ("add_far", 0),
    ("return",),
    ("add_far", 1),
    ("add_near", 3),
    ("add_far", 2),
    ("add_far", 3),
    ("loss",),
    ("logits",),
    ("add_near", 4),
    ("expr", 0),
    ("expr", 1),
    ("expr", 2),
    ("expr", 3),
    ("add_far", 4),
    ("expr", 4),
)


def halves(value):
    high = value.astype(BF16)
    return high, (value - high.astype(F32)).astype(BF16)


def product(a_high, a_low, b_high, b_low, contract):
    def one(a, b):
        return lax.dot_general(a, b, (contract, ((), ())), preferred_element_type=F32)

    return one(a_high, b_high) + (one(a_high, b_low) + one(a_low, b_high))


def plane_kernel(lines, forward_widths, backward_widths, *refs):
    chunks, turns = len(forward_widths), len(backward_widths)
    (
        (logits_ref, expr_ref, spatial_ref, count_ref, cells_ref, prior_ref),
        (pred_ref, loss_ref, glog_ref, gexp_ref),
        (lg, lq, tg, ex, pq, ab, af, ahi, alo, thi, tlo, bhi, blo, pr, sacc, s1, s2, gv, ss, rowv, rs),
        (dhi, dlo, fs, fx, fy, fz, fr, go, gs, ge, inn, l1, l2),
        (loc, ou_s, ou_r, od_s, od_r, fu_s, fu_r, fd_s, fd_r, a_s, a_r, a2_s, a2_r, r_s, r_r),
        (c_s, c_r, s1_s, s1_r, s2_s, s2_r, ss_s, ss_r, d_s, d_r, ru_s, ru_r, rd_s, rd_r),
        (f_s, f_r, fx_s, fx_r, go_s, go_r, in_s, in_r, l1_s, l1_r, l2_s, l2_r, out_s),
        bb,
        cs,
        cr,
        ds,
        es,
        ru,
        rd,
    ) = grouped(refs, (6, 4, 21, 13, 15, 14, 13, chunks, chunks, chunks, turns, turns, turns, turns))
    place = lax.axis_index("spot")
    core = lax.axis_index("gene")
    z = place // PLANE
    q = place % PLANE
    col, row = q % 2, q // 2
    mates = ((1 - row) * 2 + 1 - col, row * 2 + 1 - col, (1 - row) * 2 + col)
    others = tuple((z + step) % lines for step in range(1, lines))
    up, down = (place + PLANE, core), (place - PLANE, core)
    sibling = (place, 1 - core)
    slides, slide_rows = logits_ref.shape[0], logits_ref.shape[1]
    rows = slides * slide_rows
    cb = expr_ref.shape[0]
    genes = expr_ref.shape[1]
    last = lines - 1

    def mate(p):
        return (z * PLANE + p, core)

    def send(src, dst, send_sem, recv_sem, device):
        copy = pltpu.make_async_remote_copy(
            src_ref=src, dst_ref=dst, send_sem=send_sem, recv_sem=recv_sem, device_id=device, device_id_type=MESH
        )
        copy.start()

    def arrived(dst, recv_sem):
        pltpu.make_async_copy(dst, dst, recv_sem).wait()

    sent = arrived

    def cols(k):
        return pl.ds(sum(forward_widths[:k]), forward_widths[k])

    def turn_cols(k):
        return pl.ds(sum(backward_widths[:k]), backward_widths[k])

    def block(index):
        return pl.ds(pl.multiple_of(index * cb, cb), cb)

    def share(index):
        return pl.ds(pl.multiple_of(index * rows, rows), rows)

    def half(index):
        return pl.ds(pl.multiple_of(index * slide_rows, slide_rows), slide_rows)

    for m in range(slides):
        pltpu.make_async_copy(logits_ref.at[m], lg.at[half(m)], loc.at[m]).start()
        pltpu.make_async_copy(spatial_ref.at[m], tg.at[half(m)], loc.at[slides + m]).start()
    pltpu.make_async_copy(expr_ref, ex, loc.at[2 * slides]).start()

    barrier = pltpu.get_barrier_semaphore()
    for p in mates:
        pl.semaphore_signal(barrier, inc=1, device_id=mate(p), device_id_type=MESH)
    for o in others:
        pl.semaphore_signal(barrier, inc=1, device_id=(o * PLANE + q, core), device_id_type=MESH)
    pl.semaphore_signal(barrier, inc=1, device_id=sibling, device_id_type=MESH)
    pl.semaphore_wait(barrier, len(mates) + len(others) + 1)

    for m in range(slides):
        pltpu.make_async_copy(logits_ref.at[m], lg.at[half(m)], loc.at[m]).wait()
    for p in range(PLANE):
        for line in range(lines):
            lq[p, :, pl.ds(line * cb, cb)] = lg[half(core), pl.ds((line * PLANE + p) * cb, cb)]
    for p in mates:
        send(lq.at[p], ab.at[q, half(core)], a_s, a_r.at[q], mate(p))

    pltpu.make_async_copy(expr_ref, ex, loc.at[2 * slides]).wait()
    for k in range(chunks):
        bb[k][block(z), :] = ex[:, cols(k)]

    def own_up(k):
        here = bb[k].at[block(z)]
        send(here, here, ou_s.at[k], ou_r.at[k], up)

    def own_down(k):
        here = bb[k].at[block(z)]
        send(here, here, od_s.at[k], od_r.at[k], down)

    def low(at):
        return 2 * at < lines

    for at in range(lines):

        @pl.when(z == at)
        def _():
            for k in range(chunks):
                if at < last and (not low(at) or at == 0 or k < LEAD):
                    own_up(k)
                if at > 0 and (low(at) or at == last or k < LEAD):
                    own_down(k)

    def from_below(k, at):
        arrived(bb[k].at[pl.ds((at - 1) * cb, cb)], ou_r.at[k])
        if at > 1:
            arrived(bb[k].at[pl.ds(0, (at - 1) * cb)], fu_r.at[k])

    def from_above(k, at):
        arrived(bb[k].at[pl.ds((at + 1) * cb, cb)], od_r.at[k])
        if at < last - 1:
            arrived(bb[k].at[pl.ds((at + 2) * cb, (last - 1 - at) * cb)], fd_r.at[k])

    def upward(k, at):
        from_below(k, at)
        here = bb[k].at[pl.ds(0, at * cb)]
        send(here, here, fu_s.at[k], fu_r.at[k], up)

    def downward(k, at):
        from_above(k, at)
        here = bb[k].at[pl.ds((at + 1) * cb, (last - at) * cb)]
        send(here, here, fd_s.at[k], fd_r.at[k], down)

    def forward_far(k):
        for at in range(1, last):

            @pl.when(z == at)
            def _():
                (upward if low(at) else downward)(k, at)
                if k + LEAD < chunks:
                    (own_up if low(at) else own_down)(k + LEAD)

    def forward_near(k):
        for at in range(1, last):

            @pl.when(z == at)
            def _():
                (downward if low(at) else upward)(k, at)

    def gathered(k):
        @pl.when(z == 0)
        def _():
            from_above(k, 0)

        @pl.when(z == last)
        def _():
            from_below(k, last)

    weights = prior_ref[...].astype(F32) / fixed_point

    @pl.loop(0, rows // STEP_ROWS)
    def _(step):
        at = pl.ds(pl.multiple_of(step * STEP_ROWS, STEP_ROWS), STEP_ROWS)
        value = lg[at, :]
        peak = jnp.max(value, axis=1, keepdims=True)
        raised = jnp.exp(value - peak)
        scale = 1.0 / jnp.sum(raised, axis=1, keepdims=True)
        probs = raised * scale
        mass_rows = jnp.sum(probs * weights, axis=1, keepdims=True)
        rowv[0, at, :] = jnp.broadcast_to(mass_rows, (STEP_ROWS, LANES))
        rowv[1, at, :] = jnp.broadcast_to(peak, (STEP_ROWS, LANES))
        rowv[2, at, :] = jnp.broadcast_to(scale, (STEP_ROWS, LANES))
        for p in range(PLANE):
            for line in range(lines):
                at_cells = (line * PLANE + p) * cb
                pq[p, at, pl.ds(line * cb, cb)] = probs[:, at_cells : at_cells + cb]

    wide = lax.broadcasted_iota(jnp.int32, (rows, LANES), 1)
    rs[q] = jnp.where(wide == 0, rowv[1], rowv[2]).T[0:8]
    for p in mates:
        send(rs.at[q], rs.at[q], r_s, r_r.at[q], mate(p))

    rid = lax.broadcasted_iota(jnp.int32, (rows, 1), 0)
    first = rid < slide_rows
    position = place * slide_rows + jnp.where(first, rid, rid - slide_rows)
    count = jnp.where(first, count_ref[0], count_ref[1])
    valid = (position < count).astype(F32)
    scale_count = count.astype(F32)
    square = (slide_rows, slide_rows)
    eye = lax.broadcasted_iota(jnp.int32, square, 0) == lax.broadcasted_iota(jnp.int32, square, 1)
    counted = jnp.concatenate(
        [
            jnp.sum(jnp.where(eye, cells_ref[m : m + 1, :].astype(F32), 0.0), axis=1, keepdims=True)
            for m in range(slides)
        ],
        axis=0,
    )
    mass = rowv[0, :, 0:1]
    kcell = valid * counted

    def by_slide(value):
        return [jnp.sum(value[m * slide_rows : (m + 1) * slide_rows], axis=0, keepdims=True) for m in range(slides)]

    mass_parts = by_slide(valid * mass)
    cell_parts = by_slide(kcell)
    lane = lax.broadcasted_iota(jnp.int32, (1, LANES), 1)
    scalars = jnp.zeros((1, LANES), F32)
    for at, value in enumerate(mass_parts + cell_parts):
        scalars = jnp.where(lane == at, value, scalars)
    for m in range(slides):
        pltpu.make_async_copy(spatial_ref.at[m], tg.at[half(m)], loc.at[slides + m]).wait()
    sacc[...] = jnp.zeros_like(sacc)
    s1[q, 3 * slides :, :] = jnp.zeros((8 - 3 * slides, genes), F32)
    s1[q, 3 * slides : 3 * slides + 1, 0:LANES] = scalars

    def share_logits():
        for p in (mates[1], mates[2], mates[0]):
            here = ab.at[p, half(core)]
            arrived(here, a_r.at[p])
            send(here, here, a2_s, a2_r.at[p], sibling)

    def take_probs():
        af[q] = pq[q]
        ahi[share(q), :], alo[share(q), :] = halves(pq[q])
        for p in (mates[1], mates[2], mates[0]):
            arrived(rs.at[p], r_r.at[p])
            arrived(ab.at[p, half(1 - core)], a2_r.at[p])
            by_row = rs[p].T
            probs = jnp.exp(ab[p] - by_row[:, 0:1]) * by_row[:, 1:2]
            af[p] = probs
            ahi[share(p), :], alo[share(p), :] = halves(probs)

    def transpose(part):
        for p in (2 * part, 2 * part + 1):
            high, low_part = halves(af[p].T)
            thi[:, share(p)], tlo[:, share(p)] = high, low_part

    def forward_product(k):
        high, low = halves(bb[k][...])
        bhi[:, cols(k)], blo[:, cols(k)] = high, low
        cs[k][...] = product(ahi[...], alo[...], high, low, ((1,), (0,)))
        for p in mates:
            send(cs[k].at[share(p)], cr[k].at[q], c_s.at[k], c_r.at[k, q], mate(p))

    def finish_pred(k):
        total = cs[k][share(q), :]
        for p in mates:
            arrived(cr[k].at[p], c_r.at[k, p])
            total = total + cr[k][p]
        pr[:, cols(k)] = total
        truth = tg[:, cols(k)]
        for at, value in enumerate((total * truth, total * total, truth * truth)):
            sacc[at] += lane_groups(value)
        kept = valid * total
        stats = by_slide(kept * truth) + by_slide(kept * total) + by_slide(valid * truth * truth)
        s1[q, 0 : 3 * slides, cols(k)] = jnp.concatenate(stats, axis=0)

    early = sum(forward_widths[:EARLY])
    parts = (pl.ds(0, early), pl.ds(early, genes - early))

    def sum_plane(at):
        for p in mates:
            send(s1.at[q, :, parts[at]], s1.at[q, :, parts[at]], s1_s, s1_r.at[at, q], mate(p))

    def sum_line(at):
        for p in mates:
            arrived(s1.at[p, :, parts[at]], s1_r.at[at, p])
        s2[z, :, parts[at]] = (s1[0, :, parts[at]] + s1[1, :, parts[at]]) + (s1[2, :, parts[at]] + s1[3, :, parts[at]])
        for o in others:
            send(s2.at[z, :, parts[at]], s2.at[z, :, parts[at]], s2_s, s2_r.at[at, z], (o * PLANE + q, core))

    def sum_cores():
        sums = [jnp.sum(sacc[at], axis=1, keepdims=True) for at in range(3)]
        ss[core] = jnp.where(wide == 0, sums[0], jnp.where(wide == 1, sums[1], sums[2]))
        send(ss.at[core], ss.at[core], ss_s, ss_r, sibling)

    steps = {
        "far": forward_far,
        "near": forward_near,
        "share": share_logits,
        "take": take_probs,
        "whole": gathered,
        "product": forward_product,
        "sum": finish_pred,
        "turn": transpose,
        "plane": sum_plane,
        "cores": sum_cores,
        "line": sum_line,
    }
    for name, *where in FORWARD_STEPS:
        steps[name](*where)

    for m in range(slides):
        pltpu.make_async_copy(pr.at[half(m)], pred_ref.at[m], out_s.at[m]).start()
    arrived(ss.at[1 - core], ss_r)
    spot = ss[0] + ss[1]
    spot_dot, spot_pred, spot_true = spot[:, 0:1], spot[:, 1:2], spot[:, 2:3]
    spot_inv = lax.rsqrt(spot_pred * spot_true + tiny)
    cos_spot = spot_dot * spot_inv
    spot_back = cos_spot * spot_true / (spot_pred * spot_true + tiny)
    for o in others:
        for at in range(2):
            arrived(s2.at[o, :, parts[at]], s2_r.at[at, o])
    total = s2[0]
    for line in range(1, lines):
        total = total + s2[line]
    gene_dot, gene_pred, gene_true = total[0:2], total[2:4], total[4:6]
    gene_inv = lax.rsqrt(gene_pred * gene_true + tiny)
    cos_gene = gene_dot * gene_inv
    gv[0:2, :] = gene_inv
    gv[2:4, :] = cos_gene * gene_true / (gene_pred * gene_true + tiny)

    sacc[0] = jnp.zeros_like(sacc[0])

    def send_grad(k):
        pieces = []
        for m in range(slides):
            lo, hi = m * slide_rows, (m + 1) * slide_rows
            truth, guess = tg[lo:hi, turn_cols(k)], pr[lo:hi, turn_cols(k)]
            inverse, back = gv[m : m + 1, turn_cols(k)], gv[2 + m : 3 + m, turn_cols(k)]
            pieces.append(
                -valid[lo:hi]
                * (truth * (inverse + spot_inv[lo:hi]) - guess * back - guess * spot_back[lo:hi])
            )
        grad = jnp.concatenate(pieces, axis=0)
        here = ds[k].at[share(q)]
        here[...] = grad
        for p in mates:
            send(here, here, d_s.at[k], d_r.at[k, q], mate(p))
        sacc[0] += lane_groups(grad * pr[:, turn_cols(k)])

    gene_sum = jnp.sum(jnp.sum(cos_gene, axis=1, keepdims=True), axis=0, keepdims=True)

    mass_total = jnp.where(first, total[6:7, 0:1], total[6:7, 1:2])
    cell_total = jnp.where(first, total[6:7, 2:3], total[6:7, 3:4])
    portion = kcell / cell_total
    kl_rows = portion * (jnp.log(counted) - jnp.log(cell_total) - jnp.log(mass) + jnp.log(mass_total))
    dmass = scale_count * valid * (1.0 / mass_total - portion / mass)
    terms = jnp.sum(scale_count * kl_rows - valid * cos_spot, axis=0, keepdims=True)

    def send_terms():
        l1[q] = jnp.broadcast_to(terms, (8, LANES))
        for p in mates:
            send(l1.at[q], l1.at[q], l1_s, l1_r.at[q], mate(p))
        inner = jnp.sum(sacc[0], axis=1, keepdims=True)
        inn[core] = jnp.where(wide == 0, inner, gene_sum)
        send(inn.at[core], inn.at[core], in_s, in_r, sibling)
        rowv[1] = jnp.broadcast_to(dmass, (rows, LANES))


    def backward_product(k):
        for p in mates:
            arrived(ds[k].at[share(p)], d_r.at[k, p])
        high, low = halves(ds[k][...])
        dhi[:, turn_cols(k)], dlo[:, turn_cols(k)] = high, low
        es[k][...] = product(thi[...], tlo[...], high, low, ((1,), (0,)))

        @pl.when(z == 0)
        def _():
            if whole(k):
                pass_up(k, 1, last)
            else:
                for line in range(last, 0, -1):
                    pass_up(k, line, 1)

        @pl.when(z == last)
        def _():
            if whole(k):
                pass_down(k, 0, last)
            else:
                for line in range(last):
                    pass_down(k, line, 1)

    def whole(k):
        return k < turns - SPLIT

    def pass_up(k, line, count):
        here = pl.ds(line * cb, count * cb)
        send(es[k].at[here], ru[k].at[here], ru_s.at[k], ru_r.at[k, 0 if whole(k) else line], up)

    def pass_down(k, line, count):
        here = pl.ds(line * cb, count * cb)
        send(es[k].at[here], rd[k].at[here], rd_s.at[k], rd_r.at[k, 0 if whole(k) else line], down)

    def take_up(k, line, count):
        here = pl.ds(line * cb, count * cb)
        arrived(ru[k].at[here], ru_r.at[k, 0 if whole(k) else line])

    def take_down(k, line, count):
        here = pl.ds(line * cb, count * cb)
        arrived(rd[k].at[here], rd_r.at[k, 0 if whole(k) else line])

    def rising(k, at):
        if whole(k):
            take_up(k, at, lines - at)
            above = pl.ds((at + 1) * cb, (last - at) * cb)
            es[k][above, :] += ru[k][above, :]
            pass_up(k, at + 1, last - at)
        else:
            for line in range(last, at, -1):
                take_up(k, line, 1)
                here = pl.ds(line * cb, cb)
                es[k][here, :] += ru[k][here, :]
                pass_up(k, line, 1)

    def falling(k, at):
        if whole(k):
            take_down(k, 0, at + 1)
            below = pl.ds(0, at * cb)
            es[k][below, :] += rd[k][below, :]
            pass_down(k, 0, at)
        else:
            for line in range(at):
                take_down(k, line, 1)
                here = pl.ds(line * cb, cb)
                es[k][here, :] += rd[k][here, :]
                pass_down(k, line, 1)

    def add_near(k):
        for at in range(1, last):

            @pl.when(z == at)
            def _():
                (rising if low(at) else falling)(k, at)

    def add_far(k):
        for at in range(1, last):

            @pl.when(z == at)
            def _():
                (falling if low(at) else rising)(k, at)

    def finish_expr(k):
        for at in range(lines):

            @pl.when(z == at)
            def _():
                own = pl.ds(at * cb, cb)
                total = es[k][own, :]
                if at > 0:
                    if at == last or not whole(k):
                        take_up(k, at, 1)
                    total = total + ru[k][own, :]
                if at < last:
                    if at == 0 or not whole(k):
                        take_down(k, at, 1)
                    total = total + rd[k][own, :]
                ge[:, turn_cols(k)] = total

    def probs_gradient(k):
        at = turn_cols(k)
        part = product(dhi[:, at], dlo[:, at], bhi[:, at], blo[:, at], ((1,), (1,)))
        if k == 0:
            fs[...] = part
        else:
            fs[...] += part

    def slide_of(p, m):
        return pl.ds(pl.multiple_of(p * rows + m * slide_rows, slide_rows), slide_rows)

    def sum_probs_cores():
        for p in mates + (q,):
            fx[p] = fs[slide_of(p, 1 - core), :]
            send(fx.at[p], fy.at[p], fx_s, fx_r.at[p], sibling)

    def return_probs():
        for p in mates + (q,):
            arrived(fy.at[p], fx_r.at[p])
            fz[p] = fs[slide_of(p, core), :] + fy[p]
        for p in mates:
            send(fz.at[p], fr.at[q], f_s, f_r.at[q], mate(p))
        fr[q] = fz[q]

    def pass_terms():
        for p in mates:
            arrived(l1.at[p], l1_r.at[p])
        l2[z] = (l1[0] + l1[1]) + (l1[2] + l1[3])
        for o in others:
            send(l2.at[z], l2.at[z], l2_s, l2_r.at[z], (o * PLANE + q, core))

    def finish_logits():
        arrived(inn.at[1 - core], in_r)
        rowv[2] = (inn[0] + inn[1]) + rowv[1] * rowv[0]
        for p in mates:
            arrived(fr.at[p], f_r.at[p])
        for m in range(2):

            @pl.loop(0, slide_rows // STEP_ROWS // 2)
            def _(step):
                row_at = (m * (slide_rows // STEP_ROWS // 2) + step) * STEP_ROWS
                at = pl.ds(pl.multiple_of(row_at, STEP_ROWS), STEP_ROWS)
                whole_at = pl.ds(pl.multiple_of(core * slide_rows + row_at, STEP_ROWS), STEP_ROWS)
                by_mass, total_inner = rowv[1, whole_at, 0:1], rowv[2, whole_at, 0:1]
                for p in range(PLANE):
                    for line in range(lines):
                        here, there = pl.ds(line * cb, cb), (line * PLANE + p) * cb
                        grad = fr[p, at, here] + by_mass * weights[:, there : there + cb]
                        go[at, pl.ds(there, cb)] = pq[p, whole_at, here] * (grad - total_inner)

            part = pl.ds(m * (slide_rows // 2), slide_rows // 2)
            send(go.at[part], gs.at[part], go_s, go_r.at[m], sibling)
        pltpu.make_async_copy(go, glog_ref.at[core], out_s.at[slides + 1]).start()

    steps = {
        "grad": send_grad,
        "terms": send_terms,
        "product": backward_product,
        "probs": probs_gradient,
        "cores": sum_probs_cores,
        "return": return_probs,
        "loss": pass_terms,
        "logits": finish_logits,
        "add_near": add_near,
        "add_far": add_far,
        "expr": finish_expr,
    }
    for name, *where in BACKWARD_STEPS:
        steps[name](*where)
    pltpu.make_async_copy(ge, gexp_ref, out_s.at[slides]).start()

    for o in others:
        arrived(l2.at[o], l2_r.at[o])
    loss = l2[0]
    for line in range(1, lines):
        loss = loss + l2[line]
    loss_ref[...] = loss[0:1, 0:1] - (inn[0, 0:1, 1:2] + inn[1, 0:1, 1:2])
    for m in range(2):
        arrived(gs.at[pl.ds(m * (slide_rows // 2), slide_rows // 2)], go_r.at[m])
    pltpu.make_async_copy(gs, glog_ref.at[1 - core], out_s.at[slides + 2]).start()

    for m in range(slides):
        pltpu.make_async_copy(pr.at[half(m)], pred_ref.at[m], out_s.at[m]).wait()
    pltpu.make_async_copy(ge, gexp_ref, out_s.at[slides]).wait()
    pltpu.make_async_copy(go, glog_ref.at[core], out_s.at[slides + 1]).wait()
    pltpu.make_async_copy(gs, glog_ref.at[1 - core], out_s.at[slides + 2]).wait()
    for k in range(chunks):

        @pl.when(z < last)
        def _():
            sent(bb[k].at[block(z)], ou_s.at[k])

        @pl.when(z > 0)
        def _():
            sent(bb[k].at[block(z)], od_s.at[k])

        for at in range(1, last):

            @pl.when(z == at)
            def _():
                sent(bb[k].at[pl.ds(0, at * cb)], fu_s.at[k])
                sent(bb[k].at[pl.ds((at + 1) * cb, (last - at) * cb)], fd_s.at[k])

    for k in range(turns):
        for at in range(lines):

            @pl.when(z == at)
            def _():
                if at < last:
                    sent(es[k].at[pl.ds((at + 1) * cb, (last - at) * cb)], ru_s.at[k])
                if at > 0:
                    sent(es[k].at[pl.ds(0, at * cb)], rd_s.at[k])

    three = pl.ds(0, len(mates))
    sent(ab.at[three, half(0)], a_s)
    sent(ab.at[three, half(0)], a2_s)
    sent(rs.at[three], r_s)
    for k in range(chunks):
        sent(cr[k].at[three], c_s.at[k])
    sent(s1.at[three], s1_s)
    sent(s2.at[pl.ds(0, last)], s2_s)
    sent(ss.at[0], ss_s)
    for k in range(turns):
        sent(ds[k].at[pl.ds(0, len(mates) * rows)], d_s.at[k])
    sent(inn.at[0], in_s)
    sent(l1.at[three], l1_s)
    sent(l2.at[pl.ds(0, last)], l2_s)
    sent(fr.at[three], f_s)
    sent(fx, fx_s)
    sent(go, go_s)


def lane_groups(value):
    parts = [value[:, at : at + LANES] for at in range(0, value.shape[1], LANES)]
    return functools.reduce(lambda a, b: a + b, parts)


def grouped(refs, sizes):
    at = 0
    for size in sizes:
        yield refs[at : at + size]
        at += size


def deliver(pred_in, glog_in, gexp_in, pred_ref, glog_ref, gexp_ref, pred_mid, glog_mid, gexp_mid, sems):
    triples = ((glog_in, glog_mid, glog_ref), (pred_in, pred_mid, pred_ref), (gexp_in, gexp_mid, gexp_ref))
    loads = [pltpu.make_async_copy(src, mid, sems.at[0, at]) for at, (src, mid, _) in enumerate(triples)]
    stores = [pltpu.make_async_copy(mid, dst, sems.at[1, at]) for at, (_, mid, dst) in enumerate(triples)]
    for load in loads:
        load.start()
    for load, store in zip(loads, stores):
        load.wait()
        store.start()
    for store in stores:
        store.wait()


def plane_call(logits, expr, spatial, slide_spots, spot_cells, cell_prior, lines):
    slides, slide_rows, cells = logits.shape
    rows = slides * slide_rows
    cb, genes = expr.shape
    quarter = lines * cb
    spots = PLANE * rows
    chunks, turns = len(FORWARD), len(BACKWARD)
    dma = pltpu.SemaphoreType.DMA
    vmem = pltpu.VMEM
    anywhere = pl.BlockSpec(memory_space=pl.ANY)
    in_vmem = pl.BlockSpec(memory_space=pltpu.VMEM)
    in_smem = pl.BlockSpec(memory_space=pltpu.SMEM)
    scratch = [
        vmem((rows, cells), F32),
        vmem((PLANE, slide_rows, quarter), F32),
        vmem((rows, genes), F32),
        vmem((cb, genes), F32),
        vmem((PLANE, rows, quarter), F32),
        vmem((PLANE, rows, quarter), F32),
        vmem((PLANE, rows, quarter), F32),
        vmem((spots, quarter), BF16),
        vmem((spots, quarter), BF16),
        vmem((quarter, spots), BF16),
        vmem((quarter, spots), BF16),
        vmem((quarter, genes), BF16),
        vmem((quarter, genes), BF16),
        vmem((rows, genes), F32),
        vmem((3, rows, LANES), F32),
        vmem((PLANE, 8, genes), F32),
        vmem((lines, 8, genes), F32),
        vmem((8, genes), F32),
        vmem((2, rows, LANES), F32),
        vmem((3, rows, LANES), F32),
        vmem((PLANE, 8, rows), F32),
        vmem((spots, genes), BF16),
        vmem((spots, genes), BF16),
        vmem((spots, quarter), F32),
        vmem((PLANE, slide_rows, quarter), F32),
        vmem((PLANE, slide_rows, quarter), F32),
        vmem((PLANE, slide_rows, quarter), F32),
        vmem((PLANE, slide_rows, quarter), F32),
        vmem((slide_rows, cells), F32),
        vmem((slide_rows, cells), F32),
        vmem((cb, genes), F32),
        vmem((2, rows, LANES), F32),
        vmem((PLANE, 8, LANES), F32),
        vmem((lines, 8, LANES), F32),
        dma((2 * slides + 1,)),
        dma((chunks,)),
        dma((chunks,)),
        dma((chunks,)),
        dma((chunks,)),
        dma((chunks,)),
        dma((chunks,)),
        dma((chunks,)),
        dma((chunks,)),
        dma,
        dma((PLANE,)),
        dma,
        dma((PLANE,)),
        dma,
        dma((PLANE,)),
        dma((chunks,)),
        dma((chunks, PLANE)),
        dma,
        dma((2, PLANE)),
        dma,
        dma((2, lines)),
        dma,
        dma,
        dma((turns,)),
        dma((turns, PLANE)),
        dma((turns,)),
        dma((turns, lines)),
        dma((turns,)),
        dma((turns, lines)),
        dma,
        dma((PLANE,)),
        dma,
        dma((PLANE,)),
        dma,
        dma((2,)),
        dma,
        dma,
        dma,
        dma((PLANE,)),
        dma,
        dma((lines,)),
        dma((slides + 3,)),
    ]
    for shape, widths in (
        ((quarter,), FORWARD),
        ((spots,), FORWARD),
        ((PLANE, rows), FORWARD),
        ((spots,), BACKWARD),
        ((quarter,), BACKWARD),
        ((quarter,), BACKWARD),
        ((quarter,), BACKWARD),
    ):
        scratch += [vmem(shape + (width,), F32) for width in widths]
    pred_shape = jax.ShapeDtypeStruct((slides, slide_rows, genes), F32)
    glog_shape = jax.ShapeDtypeStruct((slides, slide_rows, cells), F32)
    gexp_shape = jax.ShapeDtypeStruct((cb, genes), F32)
    pred, loss, grad_logits, grad_expr = pl.pallas_call(
        functools.partial(plane_kernel, lines, FORWARD, BACKWARD),
        out_shape=(pred_shape, jax.ShapeDtypeStruct((1, 1), F32), glog_shape, gexp_shape),
        in_specs=[anywhere, anywhere, anywhere, in_smem, in_vmem, in_vmem],
        out_specs=(anywhere, in_vmem, anywhere, anywhere),
        scratch_shapes=scratch,
        compiler_params=pltpu.CompilerParams(
            collective_id=0, has_side_effects=True, vmem_limit_bytes=56 * 1024 * 1024
        ),
    )(logits, expr, spatial, slide_spots, spot_cells, cell_prior.reshape(1, cells))
    pred, grad_logits, grad_expr = pl.pallas_call(
        deliver,
        out_shape=(pred_shape, glog_shape, gexp_shape),
        in_specs=[anywhere] * 3,
        out_specs=(anywhere,) * 3,
        scratch_shapes=[vmem(shape.shape, F32) for shape in (pred_shape, glog_shape, gexp_shape)] + [dma((2, 3))],
        compiler_params=pltpu.CompilerParams(vmem_limit_bytes=56 * 1024 * 1024),
    )(pred, grad_logits, grad_expr)
    return pred, loss.reshape(()), grad_logits, grad_expr


def general_plan(logits, expr, spatial, slide_spots, spot_cells, cell_prior):
    place = lax.axis_index("spot")
    side = lax.axis_index("gene")
    rows_all = logits.shape[1]
    cell_rows = expr.shape[0]
    weights = cell_prior.astype(jnp.float32) / fixed_point
    gene_share = (place == 0).astype(jnp.float32)
    row_share = (side == 0).astype(jnp.float32)
    own_weights = lax.dynamic_slice_in_dim(weights, place * cell_rows, cell_rows, 0)
    expr_acc = jnp.zeros((cell_rows, expr.shape[1]), jnp.float32)
    loss_local = jnp.zeros((), jnp.float32)
    pred_list = []
    grad_list = []
    for slide in range(logits.shape[0]):
        logit_rows = logits[slide]
        counted = spot_cells[slide].astype(jnp.float32)
        target = spatial[slide]
        positions = place * rows_all + jnp.arange(rows_all, dtype=jnp.int32)
        valid = (positions < slide_spots[slide]).astype(jnp.float32)
        peak = jnp.max(logit_rows, axis=1, keepdims=True)
        raised = jnp.exp(logit_rows - peak)
        probs = raised / jnp.sum(raised, axis=1, keepdims=True)
        mass = jnp.dot(probs, weights, precision=lax.Precision.HIGHEST)
        blocks = lax.all_to_all(probs, "spot", split_axis=1, concat_axis=0, tiled=True)
        pred = lax.psum_scatter(
            jnp.dot(blocks, expr, precision=lax.Precision.HIGHEST),
            "spot",
            scatter_dimension=0,
            tiled=True,
        )
        gene_dot = jnp.sum(valid[:, None] * pred * target, axis=0)
        gene_pred = jnp.sum(valid[:, None] * pred * pred, axis=0)
        gene_true = jnp.sum(valid[:, None] * target * target, axis=0)
        mass_part = jnp.sum(valid * mass)
        kcell = valid * counted
        cell_part = jnp.sum(kcell)
        spot_dot = jnp.sum(pred * target, axis=1)
        spot_pred = jnp.sum(pred * pred, axis=1)
        spot_true = jnp.sum(target * target, axis=1)
        gene_dot, gene_pred, gene_true, mass_total, cell_total = lax.psum(
            (gene_dot, gene_pred, gene_true, mass_part, cell_part), "spot"
        )
        spot_dot, spot_pred, spot_true = lax.psum((spot_dot, spot_pred, spot_true), "gene")
        gene_inv = lax.rsqrt(gene_pred * gene_true + tiny)
        cos_gene = gene_dot * gene_inv
        spot_inv = lax.rsqrt(spot_pred * spot_true + tiny)
        cos_spot = spot_dot * spot_inv
        share = kcell / cell_total
        scale_count = slide_spots[slide].astype(jnp.float32)
        kl_part = jnp.sum(
            share * (jnp.log(counted) - jnp.log(cell_total) - jnp.log(mass) + jnp.log(mass_total))
        )
        loss_local = loss_local - gene_share * jnp.sum(cos_gene)
        loss_local = loss_local + row_share * (scale_count * kl_part - jnp.sum(valid * cos_spot))
        gene_back = cos_gene * gene_true / (gene_pred * gene_true + tiny)
        spot_back = cos_spot * spot_true / (spot_pred * spot_true + tiny)
        dpred = -valid[:, None] * (
            target * (gene_inv[None, :] + spot_inv[:, None])
            - pred * gene_back[None, :]
            - pred * spot_back[:, None]
        )
        dmass = scale_count * valid * (1.0 / mass_total - share / mass)
        pred_list.append(pred)
        grads_full, mass_full = (
            lax.all_gather(dpred, "spot", axis=0, tiled=True),
            lax.all_gather(dmass, "spot", axis=0, tiled=True),
        )
        dprob_cells = jnp.dot(grads_full, expr.T, precision=lax.Precision.HIGHEST)
        dprob_cells = lax.psum(dprob_cells, "gene")
        expr_acc = expr_acc + lax.dot_general(
            blocks, grads_full, (((0,), (0,)), ((), ())), precision=lax.Precision.HIGHEST
        )
        dprob_cells = dprob_cells + mass_full[:, None] * own_weights[None, :]
        dprob_rows = lax.all_to_all(dprob_cells, "spot", split_axis=0, concat_axis=1, tiled=True)
        inner = jnp.sum(probs * dprob_rows, axis=1, keepdims=True)
        dlogit = probs * (dprob_rows - inner)
        grad_list.append(dlogit)
    loss = lax.psum(loss_local, ("spot", "gene"))
    return (jnp.stack(pred_list), loss, jnp.stack(grad_list), expr_acc)


def solution(mesh):
    places = mesh.shape["spot"]

    def on_device(logits, expr, spatial, slide_spots, spot_cells, cell_prior):
        if places == PLANE * PLANE and mesh.shape["gene"] == 2 and expr.shape[1] == sum(FORWARD):
            return plane_call(
                logits, expr, spatial, slide_spots, spot_cells, cell_prior, places // PLANE
            )
        return general_plan(logits, expr, spatial, slide_spots, spot_cells, cell_prior)

    in_specs = (
        P(None, "spot", None),
        P("spot", "gene"),
        P(None, "spot", "gene"),
        P(),
        P(None, "spot"),
        P(),
    )
    out_specs = (P(None, "spot", "gene"), P(), P(None, "spot", None), P("spot", "gene"))
    return jax.shard_map(
        on_device, mesh=mesh, in_specs=in_specs, out_specs=out_specs, check_vma=False
    )
```

```python
import functools

import jax
import jax.numpy as jnp
from jax import lax
from jax.experimental import pallas as pl
from jax.experimental.pallas import tpu as pltpu
from jax.sharding import PartitionSpec as P

tiny = 1e-06
fixed_point = 16384.0
F32 = jnp.float32
BF16 = jnp.bfloat16
MESH = pl.DeviceIdType.MESH

PLANE = 4
LANES = 128
STEP_ROWS = 16
FORWARD = (256, 256, 256, 128, 128)
BACKWARD = (128, 256, 256, 256, 128)
SPLIT = 3
LEAD = 2
FORWARD_STEPS = (
    ("far", 0),
    ("share",),
    ("far", 1),
    ("near", 0),
    ("far", 2),
    ("near", 1),
    ("take",),
    ("turn", 0),
    ("whole", 0),
    ("product", 0),
    ("far", 3),
    ("near", 2),
    ("turn", 1),
    ("whole", 1),
    ("product", 1),
    ("whole", 2),
    ("near", 3),
    ("far", 4),
    ("product", 2),
    ("whole", 3),
    ("product", 3),
    ("whole", 4),
    ("near", 4),
    ("product", 4),
    ("sum", 0),
    ("sum", 1),
    ("sum", 2),
    ("plane", 0),
    ("sum", 3),
    ("sum", 4),
    ("plane", 1),
    ("cores",),
    ("line", 0),
    ("line", 1),
)
EARLY = 3
BACKWARD_STEPS = (
    ("grad", 0),
    ("grad", 1),
    ("grad", 2),
    ("grad", 3),
    ("grad", 4),
    ("terms",),
    ("product", 0),
    ("product", 1),
    ("probs", 0),
    ("product", 2),
    ("add_near", 0),
    ("probs", 1),
    ("probs", 2),
    ("product", 3),
    ("add_near", 1),
    ("probs", 3),
    ("product", 4),
    ("probs", 4),
    ("cores",),
    ("add_near", 2),
    ("add_far", 0),
    ("return",),
    ("add_far", 1),
    ("add_near", 3),
    ("add_far", 2),
    ("add_far", 3),
    ("loss",),
    ("logits",),
    ("add_near", 4),
    ("expr", 0),
    ("expr", 1),
    ("expr", 2),
    ("expr", 3),
    ("add_far", 4),
    ("expr", 4),
)


def halves(value):
    high = value.astype(BF16)
    return high, (value - high.astype(F32)).astype(BF16)


def product(a_high, a_low, b_high, b_low, contract):
    def one(a, b):
        return lax.dot_general(a, b, (contract, ((), ())), preferred_element_type=F32)

    return one(a_high, b_high) + (one(a_high, b_low) + one(a_low, b_high))


def plane_kernel(lines, forward_widths, backward_widths, *refs):
    chunks, turns = len(forward_widths), len(backward_widths)
    (
        (logits_ref, expr_ref, spatial_ref, count_in, cells_in, prior_in),
        (pr, loss_ref, glog, ge),
        (count_ref, cells_ref, prior_ref, lg, lq, tg, ex, pq, ab, af, ahi, alo, thi, tlo, bhi, blo, sacc, s1, s2, gv, ss, rowv, rs),
        (dhi, dlo, fs, fx, fy, fz, fr, inn, l1, l2),
        (loc, ou_s, ou_r, od_s, od_r, fu_s, fu_r, fd_s, fd_r, a_s, a_r, a2_s, a2_r, r_s, r_r),
        (c_s, c_r, s1_s, s1_r, s2_s, s2_r, ss_s, ss_r, d_s, d_r, ru_s, ru_r, rd_s, rd_r),
        (f_s, f_r, fx_s, fx_r, go_s, go_r, in_s, in_r, l1_s, l1_r, l2_s, l2_r),
        bb,
        cs,
        cr,
        ds,
        es,
        ru,
        rd,
    ) = grouped(refs, (6, 4, 23, 10, 15, 14, 12, chunks, chunks, chunks, turns, turns, turns, turns))
    place = lax.axis_index("spot")
    core = lax.axis_index("gene")
    z = place // PLANE
    q = place % PLANE
    col, row = q % 2, q // 2
    mates = ((1 - row) * 2 + 1 - col, row * 2 + 1 - col, (1 - row) * 2 + col)
    others = tuple((z + step) % lines for step in range(1, lines))
    up, down = (place + PLANE, core), (place - PLANE, core)
    sibling = (place, 1 - core)
    slides, slide_rows = logits_ref.shape[0], logits_ref.shape[1]
    rows = slides * slide_rows
    cb = expr_ref.shape[0]
    genes = expr_ref.shape[1]
    last = lines - 1

    def mate(p):
        return (z * PLANE + p, core)

    def send(src, dst, send_sem, recv_sem, device):
        copy = pltpu.make_async_remote_copy(
            src_ref=src, dst_ref=dst, send_sem=send_sem, recv_sem=recv_sem, device_id=device, device_id_type=MESH
        )
        copy.start()

    def arrived(dst, recv_sem):
        pltpu.make_async_copy(dst, dst, recv_sem).wait()

    sent = arrived

    def cols(k):
        return pl.ds(sum(forward_widths[:k]), forward_widths[k])

    def turn_cols(k):
        return pl.ds(sum(backward_widths[:k]), backward_widths[k])

    def block(index):
        return pl.ds(pl.multiple_of(index * cb, cb), cb)

    def share(index):
        return pl.ds(pl.multiple_of(index * rows, rows), rows)

    def half(index):
        return pl.ds(pl.multiple_of(index * slide_rows, slide_rows), slide_rows)

    for m in range(slides):
        pltpu.make_async_copy(logits_ref.at[m], lg.at[half(m)], loc.at[m]).start()
        pltpu.make_async_copy(spatial_ref.at[m], tg.at[half(m)], loc.at[slides + m]).start()
    pltpu.make_async_copy(expr_ref, ex, loc.at[2 * slides]).start()
    small = ((prior_in, prior_ref), (count_in, count_ref), (cells_in, cells_ref))
    for at, (src, dst) in enumerate(small):
        pltpu.make_async_copy(src, dst, loc.at[2 * slides + 1 + at]).start()

    barrier = pltpu.get_barrier_semaphore()
    for p in mates:
        pl.semaphore_signal(barrier, inc=1, device_id=mate(p), device_id_type=MESH)
    for o in others:
        pl.semaphore_signal(barrier, inc=1, device_id=(o * PLANE + q, core), device_id_type=MESH)
    pl.semaphore_signal(barrier, inc=1, device_id=sibling, device_id_type=MESH)
    pl.semaphore_wait(barrier, len(mates) + len(others) + 1)

    for m in range(slides):
        pltpu.make_async_copy(logits_ref.at[m], lg.at[half(m)], loc.at[m]).wait()
    for p in range(PLANE):
        for line in range(lines):
            lq[p, :, pl.ds(line * cb, cb)] = lg[half(core), pl.ds((line * PLANE + p) * cb, cb)]
    for p in mates:
        send(lq.at[p], ab.at[q, half(core)], a_s, a_r.at[q], mate(p))

    pltpu.make_async_copy(expr_ref, ex, loc.at[2 * slides]).wait()
    for k in range(chunks):
        bb[k][block(z), :] = ex[:, cols(k)]

    def own_up(k):
        here = bb[k].at[block(z)]
        send(here, here, ou_s.at[k], ou_r.at[k], up)

    def own_down(k):
        here = bb[k].at[block(z)]
        send(here, here, od_s.at[k], od_r.at[k], down)

    def low(at):
        return 2 * at < lines

    for at in range(lines):

        @pl.when(z == at)
        def _():
            for k in range(chunks):
                if at < last and (not low(at) or at == 0 or k < LEAD):
                    own_up(k)
                if at > 0 and (low(at) or at == last or k < LEAD):
                    own_down(k)

    def from_below(k, at):
        arrived(bb[k].at[pl.ds((at - 1) * cb, cb)], ou_r.at[k])
        if at > 1:
            arrived(bb[k].at[pl.ds(0, (at - 1) * cb)], fu_r.at[k])

    def from_above(k, at):
        arrived(bb[k].at[pl.ds((at + 1) * cb, cb)], od_r.at[k])
        if at < last - 1:
            arrived(bb[k].at[pl.ds((at + 2) * cb, (last - 1 - at) * cb)], fd_r.at[k])

    def upward(k, at):
        from_below(k, at)
        here = bb[k].at[pl.ds(0, at * cb)]
        send(here, here, fu_s.at[k], fu_r.at[k], up)

    def downward(k, at):
        from_above(k, at)
        here = bb[k].at[pl.ds((at + 1) * cb, (last - at) * cb)]
        send(here, here, fd_s.at[k], fd_r.at[k], down)

    def forward_far(k):
        for at in range(1, last):

            @pl.when(z == at)
            def _():
                (upward if low(at) else downward)(k, at)
                if k + LEAD < chunks:
                    (own_up if low(at) else own_down)(k + LEAD)

    def forward_near(k):
        for at in range(1, last):

            @pl.when(z == at)
            def _():
                (downward if low(at) else upward)(k, at)

    def gathered(k):
        @pl.when(z == 0)
        def _():
            from_above(k, 0)

        @pl.when(z == last)
        def _():
            from_below(k, last)

    for at, (src, dst) in enumerate(small):
        pltpu.make_async_copy(src, dst, loc.at[2 * slides + 1 + at]).wait()
    weights = prior_ref[...].astype(F32) / fixed_point

    @pl.loop(0, rows // STEP_ROWS)
    def _(step):
        at = pl.ds(pl.multiple_of(step * STEP_ROWS, STEP_ROWS), STEP_ROWS)
        value = lg[at, :]
        peak = jnp.max(value, axis=1, keepdims=True)
        raised = jnp.exp(value - peak)
        scale = 1.0 / jnp.sum(raised, axis=1, keepdims=True)
        probs = raised * scale
        mass_rows = jnp.sum(probs * weights, axis=1, keepdims=True)
        rowv[0, at, :] = jnp.broadcast_to(mass_rows, (STEP_ROWS, LANES))
        rowv[1, at, :] = jnp.broadcast_to(peak, (STEP_ROWS, LANES))
        rowv[2, at, :] = jnp.broadcast_to(scale, (STEP_ROWS, LANES))
        for p in range(PLANE):
            for line in range(lines):
                at_cells = (line * PLANE + p) * cb
                pq[p, at, pl.ds(line * cb, cb)] = probs[:, at_cells : at_cells + cb]

    wide = lax.broadcasted_iota(jnp.int32, (rows, LANES), 1)
    rs[q] = jnp.where(wide == 0, rowv[1], rowv[2]).T[0:8]
    for p in mates:
        send(rs.at[q], rs.at[q], r_s, r_r.at[q], mate(p))

    rid = lax.broadcasted_iota(jnp.int32, (rows, 1), 0)
    first = rid < slide_rows
    position = place * slide_rows + jnp.where(first, rid, rid - slide_rows)
    count = jnp.where(first, count_ref[0], count_ref[1])
    valid = (position < count).astype(F32)
    scale_count = count.astype(F32)
    square = (slide_rows, slide_rows)
    eye = lax.broadcasted_iota(jnp.int32, square, 0) == lax.broadcasted_iota(jnp.int32, square, 1)
    counted = jnp.concatenate(
        [
            jnp.sum(jnp.where(eye, cells_ref[m : m + 1, :].astype(F32), 0.0), axis=1, keepdims=True)
            for m in range(slides)
        ],
        axis=0,
    )
    mass = rowv[0, :, 0:1]
    kcell = valid * counted

    def by_slide(value):
        return [jnp.sum(value[m * slide_rows : (m + 1) * slide_rows], axis=0, keepdims=True) for m in range(slides)]

    mass_parts = by_slide(valid * mass)
    cell_parts = by_slide(kcell)
    lane = lax.broadcasted_iota(jnp.int32, (1, LANES), 1)
    scalars = jnp.zeros((1, LANES), F32)
    for at, value in enumerate(mass_parts + cell_parts):
        scalars = jnp.where(lane == at, value, scalars)
    for m in range(slides):
        pltpu.make_async_copy(spatial_ref.at[m], tg.at[half(m)], loc.at[slides + m]).wait()
    sacc[...] = jnp.zeros_like(sacc)
    s1[q, 3 * slides :, :] = jnp.zeros((8 - 3 * slides, genes), F32)
    s1[q, 3 * slides : 3 * slides + 1, 0:LANES] = scalars

    def share_logits():
        for p in (mates[1], mates[2], mates[0]):
            here = ab.at[p, half(core)]
            arrived(here, a_r.at[p])
            send(here, here, a2_s, a2_r.at[p], sibling)

    def take_probs():
        af[q] = pq[q]
        ahi[share(q), :], alo[share(q), :] = halves(pq[q])
        for p in (mates[1], mates[2], mates[0]):
            arrived(rs.at[p], r_r.at[p])
            arrived(ab.at[p, half(1 - core)], a2_r.at[p])
            by_row = rs[p].T
            probs = jnp.exp(ab[p] - by_row[:, 0:1]) * by_row[:, 1:2]
            af[p] = probs
            ahi[share(p), :], alo[share(p), :] = halves(probs)

    def transpose(part):
        for p in (2 * part, 2 * part + 1):
            high, low_part = halves(af[p].T)
            thi[:, share(p)], tlo[:, share(p)] = high, low_part

    def forward_product(k):
        high, low = halves(bb[k][...])
        bhi[:, cols(k)], blo[:, cols(k)] = high, low
        cs[k][...] = product(ahi[...], alo[...], high, low, ((1,), (0,)))
        for p in mates:
            send(cs[k].at[share(p)], cr[k].at[q], c_s.at[k], c_r.at[k, q], mate(p))

    def finish_pred(k):
        total = cs[k][share(q), :]
        for p in mates:
            arrived(cr[k].at[p], c_r.at[k, p])
            total = total + cr[k][p]
        pr[:, cols(k)] = total
        truth = tg[:, cols(k)]
        for at, value in enumerate((total * truth, total * total, truth * truth)):
            sacc[at] += lane_groups(value)
        kept = valid * total
        stats = by_slide(kept * truth) + by_slide(kept * total) + by_slide(valid * truth * truth)
        s1[q, 0 : 3 * slides, cols(k)] = jnp.concatenate(stats, axis=0)

    early = sum(forward_widths[:EARLY])
    parts = (pl.ds(0, early), pl.ds(early, genes - early))

    def sum_plane(at):
        for p in mates:
            send(s1.at[q, :, parts[at]], s1.at[q, :, parts[at]], s1_s, s1_r.at[at, q], mate(p))

    def sum_line(at):
        for p in mates:
            arrived(s1.at[p, :, parts[at]], s1_r.at[at, p])
        s2[z, :, parts[at]] = (s1[0, :, parts[at]] + s1[1, :, parts[at]]) + (s1[2, :, parts[at]] + s1[3, :, parts[at]])
        for o in others:
            send(s2.at[z, :, parts[at]], s2.at[z, :, parts[at]], s2_s, s2_r.at[at, z], (o * PLANE + q, core))

    def sum_cores():
        sums = [jnp.sum(sacc[at], axis=1, keepdims=True) for at in range(3)]
        ss[core] = jnp.where(wide == 0, sums[0], jnp.where(wide == 1, sums[1], sums[2]))
        send(ss.at[core], ss.at[core], ss_s, ss_r, sibling)

    steps = {
        "far": forward_far,
        "near": forward_near,
        "share": share_logits,
        "take": take_probs,
        "whole": gathered,
        "product": forward_product,
        "sum": finish_pred,
        "turn": transpose,
        "plane": sum_plane,
        "cores": sum_cores,
        "line": sum_line,
    }
    for name, *where in FORWARD_STEPS:
        steps[name](*where)

    arrived(ss.at[1 - core], ss_r)
    spot = ss[0] + ss[1]
    spot_dot, spot_pred, spot_true = spot[:, 0:1], spot[:, 1:2], spot[:, 2:3]
    spot_inv = lax.rsqrt(spot_pred * spot_true + tiny)
    cos_spot = spot_dot * spot_inv
    spot_back = cos_spot * spot_true / (spot_pred * spot_true + tiny)
    for o in others:
        for at in range(2):
            arrived(s2.at[o, :, parts[at]], s2_r.at[at, o])
    total = s2[0]
    for line in range(1, lines):
        total = total + s2[line]
    gene_dot, gene_pred, gene_true = total[0:2], total[2:4], total[4:6]
    gene_inv = lax.rsqrt(gene_pred * gene_true + tiny)
    cos_gene = gene_dot * gene_inv
    gv[0:2, :] = gene_inv
    gv[2:4, :] = cos_gene * gene_true / (gene_pred * gene_true + tiny)

    sacc[0] = jnp.zeros_like(sacc[0])

    def send_grad(k):
        pieces = []
        for m in range(slides):
            lo, hi = m * slide_rows, (m + 1) * slide_rows
            truth, guess = tg[lo:hi, turn_cols(k)], pr[lo:hi, turn_cols(k)]
            inverse, back = gv[m : m + 1, turn_cols(k)], gv[2 + m : 3 + m, turn_cols(k)]
            pieces.append(
                -valid[lo:hi]
                * (truth * (inverse + spot_inv[lo:hi]) - guess * back - guess * spot_back[lo:hi])
            )
        grad = jnp.concatenate(pieces, axis=0)
        here = ds[k].at[share(q)]
        here[...] = grad
        for p in mates:
            send(here, here, d_s.at[k], d_r.at[k, q], mate(p))
        sacc[0] += lane_groups(grad * pr[:, turn_cols(k)])

    gene_sum = jnp.sum(jnp.sum(cos_gene, axis=1, keepdims=True), axis=0, keepdims=True)

    mass_total = jnp.where(first, total[6:7, 0:1], total[6:7, 1:2])
    cell_total = jnp.where(first, total[6:7, 2:3], total[6:7, 3:4])
    portion = kcell / cell_total
    kl_rows = portion * (jnp.log(counted) - jnp.log(cell_total) - jnp.log(mass) + jnp.log(mass_total))
    dmass = scale_count * valid * (1.0 / mass_total - portion / mass)
    terms = jnp.sum(scale_count * kl_rows - valid * cos_spot, axis=0, keepdims=True)

    def send_terms():
        l1[q] = jnp.broadcast_to(terms, (8, LANES))
        for p in mates:
            send(l1.at[q], l1.at[q], l1_s, l1_r.at[q], mate(p))
        inner = jnp.sum(sacc[0], axis=1, keepdims=True)
        inn[core] = jnp.where(wide == 0, inner, gene_sum)
        send(inn.at[core], inn.at[core], in_s, in_r, sibling)
        rowv[1] = jnp.broadcast_to(dmass, (rows, LANES))


    def backward_product(k):
        for p in mates:
            arrived(ds[k].at[share(p)], d_r.at[k, p])
        high, low = halves(ds[k][...])
        dhi[:, turn_cols(k)], dlo[:, turn_cols(k)] = high, low
        es[k][...] = product(thi[...], tlo[...], high, low, ((1,), (0,)))

        @pl.when(z == 0)
        def _():
            if whole(k):
                pass_up(k, 1, last)
            else:
                for line in range(last, 0, -1):
                    pass_up(k, line, 1)

        @pl.when(z == last)
        def _():
            if whole(k):
                pass_down(k, 0, last)
            else:
                for line in range(last):
                    pass_down(k, line, 1)

    def whole(k):
        return k < turns - SPLIT

    def pass_up(k, line, count):
        here = pl.ds(line * cb, count * cb)
        send(es[k].at[here], ru[k].at[here], ru_s.at[k], ru_r.at[k, 0 if whole(k) else line], up)

    def pass_down(k, line, count):
        here = pl.ds(line * cb, count * cb)
        send(es[k].at[here], rd[k].at[here], rd_s.at[k], rd_r.at[k, 0 if whole(k) else line], down)

    def take_up(k, line, count):
        here = pl.ds(line * cb, count * cb)
        arrived(ru[k].at[here], ru_r.at[k, 0 if whole(k) else line])

    def take_down(k, line, count):
        here = pl.ds(line * cb, count * cb)
        arrived(rd[k].at[here], rd_r.at[k, 0 if whole(k) else line])

    def rising(k, at):
        if whole(k):
            take_up(k, at, lines - at)
            above = pl.ds((at + 1) * cb, (last - at) * cb)
            es[k][above, :] += ru[k][above, :]
            pass_up(k, at + 1, last - at)
        else:
            for line in range(last, at, -1):
                take_up(k, line, 1)
                here = pl.ds(line * cb, cb)
                es[k][here, :] += ru[k][here, :]
                pass_up(k, line, 1)

    def falling(k, at):
        if whole(k):
            take_down(k, 0, at + 1)
            below = pl.ds(0, at * cb)
            es[k][below, :] += rd[k][below, :]
            pass_down(k, 0, at)
        else:
            for line in range(at):
                take_down(k, line, 1)
                here = pl.ds(line * cb, cb)
                es[k][here, :] += rd[k][here, :]
                pass_down(k, line, 1)

    def add_near(k):
        for at in range(1, last):

            @pl.when(z == at)
            def _():
                (rising if low(at) else falling)(k, at)

    def add_far(k):
        for at in range(1, last):

            @pl.when(z == at)
            def _():
                (falling if low(at) else rising)(k, at)

    def finish_expr(k):
        for at in range(lines):

            @pl.when(z == at)
            def _():
                own = pl.ds(at * cb, cb)
                total = es[k][own, :]
                if at > 0:
                    if at == last or not whole(k):
                        take_up(k, at, 1)
                    total = total + ru[k][own, :]
                if at < last:
                    if at == 0 or not whole(k):
                        take_down(k, at, 1)
                    total = total + rd[k][own, :]
                ge[:, turn_cols(k)] = total

    def probs_gradient(k):
        at = turn_cols(k)
        part = product(dhi[:, at], dlo[:, at], bhi[:, at], blo[:, at], ((1,), (1,)))
        if k == 0:
            fs[...] = part
        else:
            fs[...] += part

    def slide_of(p, m):
        return pl.ds(pl.multiple_of(p * rows + m * slide_rows, slide_rows), slide_rows)

    def sum_probs_cores():
        for p in mates + (q,):
            fx[p] = fs[slide_of(p, 1 - core), :]
            send(fx.at[p], fy.at[p], fx_s, fx_r.at[p], sibling)

    def return_probs():
        for p in mates + (q,):
            arrived(fy.at[p], fx_r.at[p])
            fz[p] = fs[slide_of(p, core), :] + fy[p]
        for p in mates:
            send(fz.at[p], fr.at[q], f_s, f_r.at[q], mate(p))
        fr[q] = fz[q]

    def pass_terms():
        for p in mates:
            arrived(l1.at[p], l1_r.at[p])
        l2[z] = (l1[0] + l1[1]) + (l1[2] + l1[3])
        for o in others:
            send(l2.at[z], l2.at[z], l2_s, l2_r.at[z], (o * PLANE + q, core))

    def part_of(slide, m):
        start = slide * slide_rows + m * (slide_rows // 2)
        return pl.ds(pl.multiple_of(start, slide_rows // 2), slide_rows // 2)

    def finish_logits():
        arrived(inn.at[1 - core], in_r)
        rowv[2] = (inn[0] + inn[1]) + rowv[1] * rowv[0]
        for p in mates:
            arrived(fr.at[p], f_r.at[p])
        for m in range(2):

            @pl.loop(0, slide_rows // STEP_ROWS // 2)
            def _(step):
                row_at = (m * (slide_rows // STEP_ROWS // 2) + step) * STEP_ROWS
                at = pl.ds(pl.multiple_of(row_at, STEP_ROWS), STEP_ROWS)
                whole_at = pl.ds(pl.multiple_of(core * slide_rows + row_at, STEP_ROWS), STEP_ROWS)
                by_mass, total_inner = rowv[1, whole_at, 0:1], rowv[2, whole_at, 0:1]
                for p in range(PLANE):
                    for line in range(lines):
                        here, there = pl.ds(line * cb, cb), (line * PLANE + p) * cb
                        grad = fr[p, at, here] + by_mass * weights[:, there : there + cb]
                        glog[whole_at, pl.ds(there, cb)] = pq[p, whole_at, here] * (grad - total_inner)

            here = part_of(core, m)
            send(glog.at[here], glog.at[here], go_s, go_r.at[m], sibling)

    steps = {
        "grad": send_grad,
        "terms": send_terms,
        "product": backward_product,
        "probs": probs_gradient,
        "cores": sum_probs_cores,
        "return": return_probs,
        "loss": pass_terms,
        "logits": finish_logits,
        "add_near": add_near,
        "add_far": add_far,
        "expr": finish_expr,
    }
    for name, *where in BACKWARD_STEPS:
        steps[name](*where)

    for o in others:
        arrived(l2.at[o], l2_r.at[o])
    loss = l2[0]
    for line in range(1, lines):
        loss = loss + l2[line]
    loss_ref[...] = loss[0:1, 0:1] - (inn[0, 0:1, 1:2] + inn[1, 0:1, 1:2])
    for m in range(2):
        arrived(glog.at[part_of(1 - core, m)], go_r.at[m])

    for k in range(chunks):

        @pl.when(z < last)
        def _():
            sent(bb[k].at[block(z)], ou_s.at[k])

        @pl.when(z > 0)
        def _():
            sent(bb[k].at[block(z)], od_s.at[k])

        for at in range(1, last):

            @pl.when(z == at)
            def _():
                sent(bb[k].at[pl.ds(0, at * cb)], fu_s.at[k])
                sent(bb[k].at[pl.ds((at + 1) * cb, (last - at) * cb)], fd_s.at[k])

    for k in range(turns):
        for at in range(lines):

            @pl.when(z == at)
            def _():
                if at < last:
                    sent(es[k].at[pl.ds((at + 1) * cb, (last - at) * cb)], ru_s.at[k])
                if at > 0:
                    sent(es[k].at[pl.ds(0, at * cb)], rd_s.at[k])

    three = pl.ds(0, len(mates))
    sent(ab.at[three, half(0)], a_s)
    sent(ab.at[three, half(0)], a2_s)
    sent(rs.at[three], r_s)
    for k in range(chunks):
        sent(cr[k].at[three], c_s.at[k])
    sent(s1.at[three], s1_s)
    sent(s2.at[pl.ds(0, last)], s2_s)
    sent(ss.at[0], ss_s)
    for k in range(turns):
        sent(ds[k].at[pl.ds(0, len(mates) * rows)], d_s.at[k])
    sent(inn.at[0], in_s)
    sent(l1.at[three], l1_s)
    sent(l2.at[pl.ds(0, last)], l2_s)
    sent(fr.at[three], f_s)
    sent(fx, fx_s)
    sent(glog.at[half(0)], go_s)


def lane_groups(value):
    parts = [value[:, at : at + LANES] for at in range(0, value.shape[1], LANES)]
    return functools.reduce(lambda a, b: a + b, parts)


def grouped(refs, sizes):
    at = 0
    for size in sizes:
        yield refs[at : at + size]
        at += size


def deliver(pred_in, loss_in, glog_in, gexp_in, pred_ref, loss_ref, glog_ref, gexp_ref, sems):
    slides, slide_rows = pred_ref.shape[0], pred_ref.shape[1]
    copies = [pltpu.make_async_copy(gexp_in, gexp_ref, sems.at[2 * slides])]
    for m in range(slides):
        part = pl.ds(m * slide_rows, slide_rows)
        copies.append(pltpu.make_async_copy(glog_in.at[part], glog_ref.at[m], sems.at[m]))
        copies.append(pltpu.make_async_copy(pred_in.at[part], pred_ref.at[m], sems.at[slides + m]))
    for copy in copies:
        copy.start()
    loss_ref[...] = loss_in[...]
    for copy in copies:
        copy.wait()


def plane_call(logits, expr, spatial, slide_spots, spot_cells, cell_prior, lines):
    slides, slide_rows, cells = logits.shape
    rows = slides * slide_rows
    cb, genes = expr.shape
    quarter = lines * cb
    spots = PLANE * rows
    chunks, turns = len(FORWARD), len(BACKWARD)
    dma = pltpu.SemaphoreType.DMA
    vmem = pltpu.VMEM
    anywhere = pl.BlockSpec(memory_space=pl.ANY)
    in_vmem = pl.BlockSpec(memory_space=pltpu.VMEM)
    scratch = [
        pltpu.SMEM((slides,), jnp.int32),
        vmem((slides, slide_rows), jnp.int32),
        vmem((1, cells), jnp.int32),
        vmem((rows, cells), F32),
        vmem((PLANE, slide_rows, quarter), F32),
        vmem((rows, genes), F32),
        vmem((cb, genes), F32),
        vmem((PLANE, rows, quarter), F32),
        vmem((PLANE, rows, quarter), F32),
        vmem((PLANE, rows, quarter), F32),
        vmem((spots, quarter), BF16),
        vmem((spots, quarter), BF16),
        vmem((quarter, spots), BF16),
        vmem((quarter, spots), BF16),
        vmem((quarter, genes), BF16),
        vmem((quarter, genes), BF16),
        vmem((3, rows, LANES), F32),
        vmem((PLANE, 8, genes), F32),
        vmem((lines, 8, genes), F32),
        vmem((8, genes), F32),
        vmem((2, rows, LANES), F32),
        vmem((3, rows, LANES), F32),
        vmem((PLANE, 8, rows), F32),
        vmem((spots, genes), BF16),
        vmem((spots, genes), BF16),
        vmem((spots, quarter), F32),
        vmem((PLANE, slide_rows, quarter), F32),
        vmem((PLANE, slide_rows, quarter), F32),
        vmem((PLANE, slide_rows, quarter), F32),
        vmem((PLANE, slide_rows, quarter), F32),
        vmem((2, rows, LANES), F32),
        vmem((PLANE, 8, LANES), F32),
        vmem((lines, 8, LANES), F32),
        dma((2 * slides + 4,)),
        dma((chunks,)),
        dma((chunks,)),
        dma((chunks,)),
        dma((chunks,)),
        dma((chunks,)),
        dma((chunks,)),
        dma((chunks,)),
        dma((chunks,)),
        dma,
        dma((PLANE,)),
        dma,
        dma((PLANE,)),
        dma,
        dma((PLANE,)),
        dma((chunks,)),
        dma((chunks, PLANE)),
        dma,
        dma((2, PLANE)),
        dma,
        dma((2, lines)),
        dma,
        dma,
        dma((turns,)),
        dma((turns, PLANE)),
        dma((turns,)),
        dma((turns, lines)),
        dma((turns,)),
        dma((turns, lines)),
        dma,
        dma((PLANE,)),
        dma,
        dma((PLANE,)),
        dma,
        dma((2,)),
        dma,
        dma,
        dma,
        dma((PLANE,)),
        dma,
        dma((lines,)),
    ]
    for shape, widths in (
        ((quarter,), FORWARD),
        ((spots,), FORWARD),
        ((PLANE, rows), FORWARD),
        ((spots,), BACKWARD),
        ((quarter,), BACKWARD),
        ((quarter,), BACKWARD),
        ((quarter,), BACKWARD),
    ):
        scratch += [vmem(shape + (width,), F32) for width in widths]
    in_hbm = functools.partial(pltpu.with_memory_space_constraint, memory_space=pltpu.HBM)
    results = pl.pallas_call(
        functools.partial(plane_kernel, lines, FORWARD, BACKWARD),
        out_shape=(
            vmem((rows, genes), F32),
            jax.ShapeDtypeStruct((1, 1), F32),
            vmem((rows, cells), F32),
            vmem((cb, genes), F32),
        ),
        in_specs=[anywhere] * 6,
        out_specs=(in_vmem,) * 4,
        scratch_shapes=scratch,
        compiler_params=pltpu.CompilerParams(
            collective_id=0, has_side_effects=True, vmem_limit_bytes=48 * 1024 * 1024
        ),
    )(*map(in_hbm, (logits, expr, spatial, slide_spots, spot_cells, cell_prior.reshape(1, cells))))
    pred, loss, grad_logits, grad_expr = pl.pallas_call(
        deliver,
        out_shape=(
            jax.ShapeDtypeStruct((slides, slide_rows, genes), F32),
            jax.ShapeDtypeStruct((1, 1), F32),
            jax.ShapeDtypeStruct((slides, slide_rows, cells), F32),
            jax.ShapeDtypeStruct((cb, genes), F32),
        ),
        in_specs=[anywhere, in_vmem, anywhere, anywhere],
        out_specs=(anywhere, in_vmem, anywhere, anywhere),
        scratch_shapes=[dma((2 * slides + 1,))],
    )(*results)
    return pred, loss.reshape(()), grad_logits, grad_expr


def general_plan(logits, expr, spatial, slide_spots, spot_cells, cell_prior):
    place = lax.axis_index("spot")
    side = lax.axis_index("gene")
    rows_all = logits.shape[1]
    cell_rows = expr.shape[0]
    weights = cell_prior.astype(jnp.float32) / fixed_point
    gene_share = (place == 0).astype(jnp.float32)
    row_share = (side == 0).astype(jnp.float32)
    own_weights = lax.dynamic_slice_in_dim(weights, place * cell_rows, cell_rows, 0)
    expr_acc = jnp.zeros((cell_rows, expr.shape[1]), jnp.float32)
    loss_local = jnp.zeros((), jnp.float32)
    pred_list = []
    grad_list = []
    for slide in range(logits.shape[0]):
        logit_rows = logits[slide]
        counted = spot_cells[slide].astype(jnp.float32)
        target = spatial[slide]
        positions = place * rows_all + jnp.arange(rows_all, dtype=jnp.int32)
        valid = (positions < slide_spots[slide]).astype(jnp.float32)
        peak = jnp.max(logit_rows, axis=1, keepdims=True)
        raised = jnp.exp(logit_rows - peak)
        probs = raised / jnp.sum(raised, axis=1, keepdims=True)
        mass = jnp.dot(probs, weights, precision=lax.Precision.HIGHEST)
        blocks = lax.all_to_all(probs, "spot", split_axis=1, concat_axis=0, tiled=True)
        pred = lax.psum_scatter(
            jnp.dot(blocks, expr, precision=lax.Precision.HIGHEST),
            "spot",
            scatter_dimension=0,
            tiled=True,
        )
        gene_dot = jnp.sum(valid[:, None] * pred * target, axis=0)
        gene_pred = jnp.sum(valid[:, None] * pred * pred, axis=0)
        gene_true = jnp.sum(valid[:, None] * target * target, axis=0)
        mass_part = jnp.sum(valid * mass)
        kcell = valid * counted
        cell_part = jnp.sum(kcell)
        spot_dot = jnp.sum(pred * target, axis=1)
        spot_pred = jnp.sum(pred * pred, axis=1)
        spot_true = jnp.sum(target * target, axis=1)
        gene_dot, gene_pred, gene_true, mass_total, cell_total = lax.psum(
            (gene_dot, gene_pred, gene_true, mass_part, cell_part), "spot"
        )
        spot_dot, spot_pred, spot_true = lax.psum((spot_dot, spot_pred, spot_true), "gene")
        gene_inv = lax.rsqrt(gene_pred * gene_true + tiny)
        cos_gene = gene_dot * gene_inv
        spot_inv = lax.rsqrt(spot_pred * spot_true + tiny)
        cos_spot = spot_dot * spot_inv
        share = kcell / cell_total
        scale_count = slide_spots[slide].astype(jnp.float32)
        kl_part = jnp.sum(
            share * (jnp.log(counted) - jnp.log(cell_total) - jnp.log(mass) + jnp.log(mass_total))
        )
        loss_local = loss_local - gene_share * jnp.sum(cos_gene)
        loss_local = loss_local + row_share * (scale_count * kl_part - jnp.sum(valid * cos_spot))
        gene_back = cos_gene * gene_true / (gene_pred * gene_true + tiny)
        spot_back = cos_spot * spot_true / (spot_pred * spot_true + tiny)
        dpred = -valid[:, None] * (
            target * (gene_inv[None, :] + spot_inv[:, None])
            - pred * gene_back[None, :]
            - pred * spot_back[:, None]
        )
        dmass = scale_count * valid * (1.0 / mass_total - share / mass)
        pred_list.append(pred)
        grads_full, mass_full = (
            lax.all_gather(dpred, "spot", axis=0, tiled=True),
            lax.all_gather(dmass, "spot", axis=0, tiled=True),
        )
        dprob_cells = jnp.dot(grads_full, expr.T, precision=lax.Precision.HIGHEST)
        dprob_cells = lax.psum(dprob_cells, "gene")
        expr_acc = expr_acc + lax.dot_general(
            blocks, grads_full, (((0,), (0,)), ((), ())), precision=lax.Precision.HIGHEST
        )
        dprob_cells = dprob_cells + mass_full[:, None] * own_weights[None, :]
        dprob_rows = lax.all_to_all(dprob_cells, "spot", split_axis=0, concat_axis=1, tiled=True)
        inner = jnp.sum(probs * dprob_rows, axis=1, keepdims=True)
        dlogit = probs * (dprob_rows - inner)
        grad_list.append(dlogit)
    loss = lax.psum(loss_local, ("spot", "gene"))
    return (jnp.stack(pred_list), loss, jnp.stack(grad_list), expr_acc)


def solution(mesh):
    places = mesh.shape["spot"]

    def on_device(logits, expr, spatial, slide_spots, spot_cells, cell_prior):
        if places == PLANE * PLANE and mesh.shape["gene"] == 2 and expr.shape[1] == sum(FORWARD):
            return plane_call(
                logits, expr, spatial, slide_spots, spot_cells, cell_prior, places // PLANE
            )
        return general_plan(logits, expr, spatial, slide_spots, spot_cells, cell_prior)

    in_specs = (
        P(None, "spot", None),
        P("spot", "gene"),
        P(None, "spot", "gene"),
        P(),
        P(None, "spot"),
        P(),
    )
    out_specs = (P(None, "spot", "gene"), P(), P(None, "spot", None), P("spot", "gene"))
    return jax.shard_map(
        on_device, mesh=mesh, in_specs=in_specs, out_specs=out_specs, check_vma=False
    )
```

```python
import functools

import jax
import jax.numpy as jnp
from jax import lax
from jax.experimental import pallas as pl
from jax.experimental.pallas import tpu as pltpu
from jax.sharding import PartitionSpec as P

tiny = 1e-06
fixed_point = 16384.0
F32 = jnp.float32
BF16 = jnp.bfloat16
MESH = pl.DeviceIdType.MESH

PLANE = 4
LANES = 128
STEP_ROWS = 16
FORWARD = (256, 256, 256, 128, 128)
BACKWARD = (128, 256, 256, 256, 128)
SPLIT = 3
LEAD = 2
FORWARD_STEPS = (
    ("far", 0),
    ("share",),
    ("far", 1),
    ("near", 0),
    ("far", 2),
    ("near", 1),
    ("take",),
    ("turn", 0),
    ("whole", 0),
    ("product", 0),
    ("far", 3),
    ("near", 2),
    ("turn", 1),
    ("whole", 1),
    ("product", 1),
    ("whole", 2),
    ("near", 3),
    ("far", 4),
    ("product", 2),
    ("whole", 3),
    ("product", 3),
    ("whole", 4),
    ("near", 4),
    ("product", 4),
    ("sum", 0),
    ("sum", 1),
    ("sum", 2),
    ("plane", 0),
    ("sum", 3),
    ("sum", 4),
    ("plane", 1),
    ("cores",),
    ("line", 0),
    ("line", 1),
)
EARLY = 3
BACKWARD_STEPS = (
    ("grad", 0),
    ("grad", 1),
    ("grad", 2),
    ("grad", 3),
    ("grad", 4),
    ("terms",),
    ("product", 0),
    ("product", 1),
    ("probs", 0),
    ("product", 2),
    ("add_near", 0),
    ("probs", 1),
    ("probs", 2),
    ("product", 3),
    ("add_near", 1),
    ("probs", 3),
    ("product", 4),
    ("probs", 4),
    ("cores",),
    ("add_near", 2),
    ("add_far", 0),
    ("return",),
    ("add_far", 1),
    ("add_near", 3),
    ("add_far", 2),
    ("add_far", 3),
    ("loss",),
    ("logits",),
    ("add_near", 4),
    ("expr", 0),
    ("expr", 1),
    ("expr", 2),
    ("expr", 3),
    ("add_far", 4),
    ("expr", 4),
)


def halves(value):
    high = value.astype(BF16)
    return high, (value - high.astype(F32)).astype(BF16)


def product(a_high, a_low, b_high, b_low, contract):
    def one(a, b):
        return lax.dot_general(a, b, (contract, ((), ())), preferred_element_type=F32)

    return one(a_high, b_high) + (one(a_high, b_low) + one(a_low, b_high))


def plane_kernel(lines, forward_widths, backward_widths, *refs):
    chunks, turns = len(forward_widths), len(backward_widths)
    (
        (logits_ref, expr_ref, spatial_ref, count_in, cells_in, prior_in),
        (pr, loss_ref, glog, ge),
        (count_ref, cells_ref, prior_ref, lg, lq, tg, ex, pq, ab, af, ahi, alo, thi, tlo, bhi, blo, sacc, s1, s2, gv, ss, rowv, rs),
        (dhi, dlo, fs, fx, fy, fz, fr, inn, l1, l2),
        (loc, ou_s, ou_r, od_s, od_r, fu_s, fu_r, fd_s, fd_r, a_s, a_r, a2_s, a2_r, r_s, r_r),
        (c_s, c_r, s1_s, s1_r, s2_s, s2_r, ss_s, ss_r, d_s, d_r, ru_s, ru_r, rd_s, rd_r),
        (f_s, f_r, fx_s, fx_r, go_s, go_r, in_s, in_r, l1_s, l1_r, l2_s, l2_r),
        bb,
        cs,
        cr,
        ds,
        es,
        ru,
        rd,
    ) = grouped(refs, (6, 4, 23, 10, 15, 14, 12, chunks, chunks, chunks, turns, turns, turns, turns))
    place = lax.axis_index("spot")
    core = lax.axis_index("gene")
    z = place // PLANE
    q = place % PLANE
    col, row = q % 2, q // 2
    mates = ((1 - row) * 2 + 1 - col, row * 2 + 1 - col, (1 - row) * 2 + col)
    others = tuple((z + step) % lines for step in range(1, lines))
    up, down = (place + PLANE, core), (place - PLANE, core)
    sibling = (place, 1 - core)
    slides, slide_rows = logits_ref.shape[0], logits_ref.shape[1]
    rows = slides * slide_rows
    cb = expr_ref.shape[0]
    genes = expr_ref.shape[1]
    last = lines - 1

    def mate(p):
        return (z * PLANE + p, core)

    def send(src, dst, send_sem, recv_sem, device):
        copy = pltpu.make_async_remote_copy(
            src_ref=src, dst_ref=dst, send_sem=send_sem, recv_sem=recv_sem, device_id=device, device_id_type=MESH
        )
        copy.start()

    def arrived(dst, recv_sem):
        pltpu.make_async_copy(dst, dst, recv_sem).wait()

    sent = arrived

    def cols(k):
        return pl.ds(sum(forward_widths[:k]), forward_widths[k])

    def turn_cols(k):
        return pl.ds(sum(backward_widths[:k]), backward_widths[k])

    def block(index):
        return pl.ds(pl.multiple_of(index * cb, cb), cb)

    def share(index):
        return pl.ds(pl.multiple_of(index * rows, rows), rows)

    def half(index):
        return pl.ds(pl.multiple_of(index * slide_rows, slide_rows), slide_rows)

    for m in range(slides):
        pltpu.make_async_copy(logits_ref.at[m], lg.at[half(m)], loc.at[m]).start()
        pltpu.make_async_copy(spatial_ref.at[m], tg.at[half(m)], loc.at[slides + m]).start()
    pltpu.make_async_copy(expr_ref, ex, loc.at[2 * slides]).start()
    small = ((prior_in, prior_ref), (count_in, count_ref), (cells_in, cells_ref))
    for at, (src, dst) in enumerate(small):
        pltpu.make_async_copy(src, dst, loc.at[2 * slides + 1 + at]).start()

    barrier = pltpu.get_barrier_semaphore()
    for p in mates:
        pl.semaphore_signal(barrier, inc=1, device_id=mate(p), device_id_type=MESH)
    for o in others:
        pl.semaphore_signal(barrier, inc=1, device_id=(o * PLANE + q, core), device_id_type=MESH)
    pl.semaphore_signal(barrier, inc=1, device_id=sibling, device_id_type=MESH)
    pl.semaphore_wait(barrier, len(mates) + len(others) + 1)

    for m in range(slides):
        pltpu.make_async_copy(logits_ref.at[m], lg.at[half(m)], loc.at[m]).wait()
    for p in range(PLANE):
        for line in range(lines):
            lq[p, :, pl.ds(line * cb, cb)] = lg[half(core), pl.ds((line * PLANE + p) * cb, cb)]
    for p in mates:
        send(lq.at[p], ab.at[q, half(core)], a_s, a_r.at[q], mate(p))

    pltpu.make_async_copy(expr_ref, ex, loc.at[2 * slides]).wait()
    for k in range(chunks):
        bb[k][block(z), :] = ex[:, cols(k)]

    def own_up(k):
        here = bb[k].at[block(z)]
        send(here, here, ou_s.at[k], ou_r.at[k], up)

    def own_down(k):
        here = bb[k].at[block(z)]
        send(here, here, od_s.at[k], od_r.at[k], down)

    def low(at):
        return 2 * at < lines

    for at in range(lines):

        @pl.when(z == at)
        def _():
            for k in range(chunks):
                if at < last and (not low(at) or at == 0 or k < LEAD):
                    own_up(k)
                if at > 0 and (low(at) or at == last or k < LEAD):
                    own_down(k)

    def from_below(k, at):
        arrived(bb[k].at[pl.ds((at - 1) * cb, cb)], ou_r.at[k])
        if at > 1:
            arrived(bb[k].at[pl.ds(0, (at - 1) * cb)], fu_r.at[k])

    def from_above(k, at):
        arrived(bb[k].at[pl.ds((at + 1) * cb, cb)], od_r.at[k])
        if at < last - 1:
            arrived(bb[k].at[pl.ds((at + 2) * cb, (last - 1 - at) * cb)], fd_r.at[k])

    def upward(k, at):
        from_below(k, at)
        here = bb[k].at[pl.ds(0, at * cb)]
        send(here, here, fu_s.at[k], fu_r.at[k], up)

    def downward(k, at):
        from_above(k, at)
        here = bb[k].at[pl.ds((at + 1) * cb, (last - at) * cb)]
        send(here, here, fd_s.at[k], fd_r.at[k], down)

    def forward_far(k):
        for at in range(1, last):

            @pl.when(z == at)
            def _():
                (upward if low(at) else downward)(k, at)
                if k + LEAD < chunks:
                    (own_up if low(at) else own_down)(k + LEAD)

    def forward_near(k):
        for at in range(1, last):

            @pl.when(z == at)
            def _():
                (downward if low(at) else upward)(k, at)

    def gathered(k):
        @pl.when(z == 0)
        def _():
            from_above(k, 0)

        @pl.when(z == last)
        def _():
            from_below(k, last)

    for at, (src, dst) in enumerate(small):
        pltpu.make_async_copy(src, dst, loc.at[2 * slides + 1 + at]).wait()
    weights = prior_ref[...].astype(F32) / fixed_point

    @pl.loop(0, rows // STEP_ROWS)
    def _(step):
        at = pl.ds(pl.multiple_of(step * STEP_ROWS, STEP_ROWS), STEP_ROWS)
        value = lg[at, :]
        peak = jnp.max(value, axis=1, keepdims=True)
        raised = jnp.exp(value - peak)
        scale = 1.0 / jnp.sum(raised, axis=1, keepdims=True)
        probs = raised * scale
        mass_rows = jnp.sum(probs * weights, axis=1, keepdims=True)
        rowv[0, at, :] = jnp.broadcast_to(mass_rows, (STEP_ROWS, LANES))
        rowv[1, at, :] = jnp.broadcast_to(peak, (STEP_ROWS, LANES))
        rowv[2, at, :] = jnp.broadcast_to(scale, (STEP_ROWS, LANES))
        for p in range(PLANE):
            for line in range(lines):
                at_cells = (line * PLANE + p) * cb
                pq[p, at, pl.ds(line * cb, cb)] = probs[:, at_cells : at_cells + cb]

    wide = lax.broadcasted_iota(jnp.int32, (rows, LANES), 1)
    rs[q] = jnp.where(wide == 0, rowv[1], rowv[2]).T[0:8]
    for p in mates:
        send(rs.at[q], rs.at[q], r_s, r_r.at[q], mate(p))

    rid = lax.broadcasted_iota(jnp.int32, (rows, 1), 0)
    first = rid < slide_rows
    position = place * slide_rows + jnp.where(first, rid, rid - slide_rows)
    count = jnp.where(first, count_ref[0], count_ref[1])
    valid = (position < count).astype(F32)
    scale_count = count.astype(F32)
    square = (slide_rows, slide_rows)
    eye = lax.broadcasted_iota(jnp.int32, square, 0) == lax.broadcasted_iota(jnp.int32, square, 1)
    counted = jnp.concatenate(
        [
            jnp.sum(jnp.where(eye, cells_ref[m : m + 1, :].astype(F32), 0.0), axis=1, keepdims=True)
            for m in range(slides)
        ],
        axis=0,
    )
    mass = rowv[0, :, 0:1]
    kcell = valid * counted

    def by_slide(value):
        return [jnp.sum(value[m * slide_rows : (m + 1) * slide_rows], axis=0, keepdims=True) for m in range(slides)]

    mass_parts = by_slide(valid * mass)
    cell_parts = by_slide(kcell)
    lane = lax.broadcasted_iota(jnp.int32, (1, LANES), 1)
    scalars = jnp.zeros((1, LANES), F32)
    for at, value in enumerate(mass_parts + cell_parts):
        scalars = jnp.where(lane == at, value, scalars)
    for m in range(slides):
        pltpu.make_async_copy(spatial_ref.at[m], tg.at[half(m)], loc.at[slides + m]).wait()
    sacc[...] = jnp.zeros_like(sacc)
    s1[q, 3 * slides :, :] = jnp.zeros((8 - 3 * slides, genes), F32)
    s1[q, 3 * slides : 3 * slides + 1, 0:LANES] = scalars

    def share_logits():
        for p in (mates[1], mates[2], mates[0]):
            here = ab.at[p, half(core)]
            arrived(here, a_r.at[p])
            send(here, here, a2_s, a2_r.at[p], sibling)

    def take_probs():
        af[q] = pq[q]
        ahi[share(q), :], alo[share(q), :] = halves(pq[q])
        for p in (mates[1], mates[2], mates[0]):
            arrived(rs.at[p], r_r.at[p])
            arrived(ab.at[p, half(1 - core)], a2_r.at[p])
            by_row = rs[p].T
            probs = jnp.exp(ab[p] - by_row[:, 0:1]) * by_row[:, 1:2]
            af[p] = probs
            ahi[share(p), :], alo[share(p), :] = halves(probs)

    def transpose(part):
        for p in (2 * part, 2 * part + 1):
            high, low_part = halves(af[p].T)
            thi[:, share(p)], tlo[:, share(p)] = high, low_part

    def forward_product(k):
        high, low = halves(bb[k][...])
        bhi[:, cols(k)], blo[:, cols(k)] = high, low
        cs[k][...] = product(ahi[...], alo[...], high, low, ((1,), (0,)))
        for p in mates:
            send(cs[k].at[share(p)], cr[k].at[q], c_s.at[k], c_r.at[k, q], mate(p))

    def finish_pred(k):
        total = cs[k][share(q), :]
        for p in mates:
            arrived(cr[k].at[p], c_r.at[k, p])
            total = total + cr[k][p]
        pr[:, cols(k)] = total
        truth = tg[:, cols(k)]
        for at, value in enumerate((total * truth, total * total, truth * truth)):
            sacc[at] += lane_groups(value)
        kept = valid * total
        stats = by_slide(kept * truth) + by_slide(kept * total) + by_slide(valid * truth * truth)
        s1[q, 0 : 3 * slides, cols(k)] = jnp.concatenate(stats, axis=0)

    early = sum(forward_widths[:EARLY])
    parts = (pl.ds(0, early), pl.ds(early, genes - early))

    def sum_plane(at):
        for p in mates:
            send(s1.at[q, :, parts[at]], s1.at[q, :, parts[at]], s1_s, s1_r.at[at, q], mate(p))

    def sum_line(at):
        for p in mates:
            arrived(s1.at[p, :, parts[at]], s1_r.at[at, p])
        s2[z, :, parts[at]] = (s1[0, :, parts[at]] + s1[1, :, parts[at]]) + (s1[2, :, parts[at]] + s1[3, :, parts[at]])
        for o in others:
            send(s2.at[z, :, parts[at]], s2.at[z, :, parts[at]], s2_s, s2_r.at[at, z], (o * PLANE + q, core))

    def sum_cores():
        sums = [jnp.sum(sacc[at], axis=1, keepdims=True) for at in range(3)]
        ss[core] = jnp.where(wide == 0, sums[0], jnp.where(wide == 1, sums[1], sums[2]))
        send(ss.at[core], ss.at[core], ss_s, ss_r, sibling)

    steps = {
        "far": forward_far,
        "near": forward_near,
        "share": share_logits,
        "take": take_probs,
        "whole": gathered,
        "product": forward_product,
        "sum": finish_pred,
        "turn": transpose,
        "plane": sum_plane,
        "cores": sum_cores,
        "line": sum_line,
    }
    for name, *where in FORWARD_STEPS:
        steps[name](*where)

    arrived(ss.at[1 - core], ss_r)
    spot = ss[0] + ss[1]
    spot_dot, spot_pred, spot_true = spot[:, 0:1], spot[:, 1:2], spot[:, 2:3]
    spot_inv = lax.rsqrt(spot_pred * spot_true + tiny)
    cos_spot = spot_dot * spot_inv
    spot_back = cos_spot * spot_true / (spot_pred * spot_true + tiny)
    for o in others:
        for at in range(2):
            arrived(s2.at[o, :, parts[at]], s2_r.at[at, o])
    total = s2[0]
    for line in range(1, lines):
        total = total + s2[line]
    gene_dot, gene_pred, gene_true = total[0:2], total[2:4], total[4:6]
    gene_inv = lax.rsqrt(gene_pred * gene_true + tiny)
    cos_gene = gene_dot * gene_inv
    gv[0:2, :] = gene_inv
    gv[2:4, :] = cos_gene * gene_true / (gene_pred * gene_true + tiny)

    sacc[0] = jnp.zeros_like(sacc[0])

    def send_grad(k):
        pieces = []
        for m in range(slides):
            lo, hi = m * slide_rows, (m + 1) * slide_rows
            truth, guess = tg[lo:hi, turn_cols(k)], pr[lo:hi, turn_cols(k)]
            inverse, back = gv[m : m + 1, turn_cols(k)], gv[2 + m : 3 + m, turn_cols(k)]
            pieces.append(
                -valid[lo:hi]
                * (truth * (inverse + spot_inv[lo:hi]) - guess * back - guess * spot_back[lo:hi])
            )
        grad = jnp.concatenate(pieces, axis=0)
        here = ds[k].at[share(q)]
        here[...] = grad
        for p in mates:
            send(here, here, d_s.at[k], d_r.at[k, q], mate(p))
        sacc[0] += lane_groups(grad * pr[:, turn_cols(k)])

    gene_sum = jnp.sum(jnp.sum(cos_gene, axis=1, keepdims=True), axis=0, keepdims=True)

    mass_total = jnp.where(first, total[6:7, 0:1], total[6:7, 1:2])
    cell_total = jnp.where(first, total[6:7, 2:3], total[6:7, 3:4])
    portion = kcell / cell_total
    kl_rows = portion * (jnp.log(counted) - jnp.log(cell_total) - jnp.log(mass) + jnp.log(mass_total))
    dmass = scale_count * valid * (1.0 / mass_total - portion / mass)
    terms = jnp.sum(scale_count * kl_rows - valid * cos_spot, axis=0, keepdims=True)

    def send_terms():
        l1[q] = jnp.broadcast_to(terms, (8, LANES))
        for p in mates:
            send(l1.at[q], l1.at[q], l1_s, l1_r.at[q], mate(p))
        inner = jnp.sum(sacc[0], axis=1, keepdims=True)
        inn[core] = jnp.where(wide == 0, inner, gene_sum)
        send(inn.at[core], inn.at[core], in_s, in_r, sibling)
        rowv[1] = jnp.broadcast_to(dmass, (rows, LANES))


    def backward_product(k):
        for p in mates:
            arrived(ds[k].at[share(p)], d_r.at[k, p])
        high, low = halves(ds[k][...])
        dhi[:, turn_cols(k)], dlo[:, turn_cols(k)] = high, low
        es[k][...] = product(thi[...], tlo[...], high, low, ((1,), (0,)))

        @pl.when(z == 0)
        def _():
            if whole(k):
                pass_up(k, 1, last)
            else:
                for line in range(last, 0, -1):
                    pass_up(k, line, 1)

        @pl.when(z == last)
        def _():
            if whole(k):
                pass_down(k, 0, last)
            else:
                for line in range(last):
                    pass_down(k, line, 1)

    def whole(k):
        return k < turns - SPLIT

    def pass_up(k, line, count):
        here = pl.ds(line * cb, count * cb)
        send(es[k].at[here], ru[k].at[here], ru_s.at[k], ru_r.at[k, 0 if whole(k) else line], up)

    def pass_down(k, line, count):
        here = pl.ds(line * cb, count * cb)
        send(es[k].at[here], rd[k].at[here], rd_s.at[k], rd_r.at[k, 0 if whole(k) else line], down)

    def take_up(k, line, count):
        here = pl.ds(line * cb, count * cb)
        arrived(ru[k].at[here], ru_r.at[k, 0 if whole(k) else line])

    def take_down(k, line, count):
        here = pl.ds(line * cb, count * cb)
        arrived(rd[k].at[here], rd_r.at[k, 0 if whole(k) else line])

    def rising(k, at):
        if whole(k):
            take_up(k, at, lines - at)
            above = pl.ds((at + 1) * cb, (last - at) * cb)
            es[k][above, :] += ru[k][above, :]
            pass_up(k, at + 1, last - at)
        else:
            for line in range(last, at, -1):
                take_up(k, line, 1)
                here = pl.ds(line * cb, cb)
                es[k][here, :] += ru[k][here, :]
                pass_up(k, line, 1)

    def falling(k, at):
        if whole(k):
            take_down(k, 0, at + 1)
            below = pl.ds(0, at * cb)
            es[k][below, :] += rd[k][below, :]
            pass_down(k, 0, at)
        else:
            for line in range(at):
                take_down(k, line, 1)
                here = pl.ds(line * cb, cb)
                es[k][here, :] += rd[k][here, :]
                pass_down(k, line, 1)

    def add_near(k):
        for at in range(1, last):

            @pl.when(z == at)
            def _():
                (rising if low(at) else falling)(k, at)

    def add_far(k):
        for at in range(1, last):

            @pl.when(z == at)
            def _():
                (falling if low(at) else rising)(k, at)

    def finish_expr(k):
        for at in range(lines):

            @pl.when(z == at)
            def _():
                own = pl.ds(at * cb, cb)
                total = es[k][own, :]
                if at > 0:
                    if at == last or not whole(k):
                        take_up(k, at, 1)
                    total = total + ru[k][own, :]
                if at < last:
                    if at == 0 or not whole(k):
                        take_down(k, at, 1)
                    total = total + rd[k][own, :]
                ge[:, turn_cols(k)] = total

    def probs_gradient(k):
        at = turn_cols(k)
        part = product(dhi[:, at], dlo[:, at], bhi[:, at], blo[:, at], ((1,), (1,)))
        if k == 0:
            fs[...] = part
        else:
            fs[...] += part

    def slide_of(p, m):
        return pl.ds(pl.multiple_of(p * rows + m * slide_rows, slide_rows), slide_rows)

    def sum_probs_cores():
        for p in mates + (q,):
            fx[p] = fs[slide_of(p, 1 - core), :]
            send(fx.at[p], fy.at[p], fx_s, fx_r.at[p], sibling)

    def return_probs():
        for p in mates + (q,):
            arrived(fy.at[p], fx_r.at[p])
            fz[p] = fs[slide_of(p, core), :] + fy[p]
        for p in mates:
            send(fz.at[p], fr.at[q], f_s, f_r.at[q], mate(p))
        fr[q] = fz[q]

    def pass_terms():
        for p in mates:
            arrived(l1.at[p], l1_r.at[p])
        l2[z] = (l1[0] + l1[1]) + (l1[2] + l1[3])
        for o in others:
            send(l2.at[z], l2.at[z], l2_s, l2_r.at[z], (o * PLANE + q, core))

    def part_of(slide, m):
        start = slide * slide_rows + m * (slide_rows // 2)
        return pl.ds(pl.multiple_of(start, slide_rows // 2), slide_rows // 2)

    def finish_logits():
        arrived(inn.at[1 - core], in_r)
        rowv[2] = (inn[0] + inn[1]) + rowv[1] * rowv[0]
        for p in mates:
            arrived(fr.at[p], f_r.at[p])
        for m in range(2):

            @pl.loop(0, slide_rows // STEP_ROWS // 2)
            def _(step):
                row_at = (m * (slide_rows // STEP_ROWS // 2) + step) * STEP_ROWS
                at = pl.ds(pl.multiple_of(row_at, STEP_ROWS), STEP_ROWS)
                whole_at = pl.ds(pl.multiple_of(core * slide_rows + row_at, STEP_ROWS), STEP_ROWS)
                by_mass, total_inner = rowv[1, whole_at, 0:1], rowv[2, whole_at, 0:1]
                for p in range(PLANE):
                    for line in range(lines):
                        here, there = pl.ds(line * cb, cb), (line * PLANE + p) * cb
                        grad = fr[p, at, here] + by_mass * weights[:, there : there + cb]
                        glog[whole_at, pl.ds(there, cb)] = pq[p, whole_at, here] * (grad - total_inner)

            here = part_of(core, m)
            send(glog.at[here], glog.at[here], go_s, go_r.at[m], sibling)

    steps = {
        "grad": send_grad,
        "terms": send_terms,
        "product": backward_product,
        "probs": probs_gradient,
        "cores": sum_probs_cores,
        "return": return_probs,
        "loss": pass_terms,
        "logits": finish_logits,
        "add_near": add_near,
        "add_far": add_far,
        "expr": finish_expr,
    }
    for name, *where in BACKWARD_STEPS:
        steps[name](*where)

    for o in others:
        arrived(l2.at[o], l2_r.at[o])
    loss = l2[0]
    for line in range(1, lines):
        loss = loss + l2[line]
    loss_ref[...] = loss[0:1, 0:1] - (inn[0, 0:1, 1:2] + inn[1, 0:1, 1:2])
    for m in range(2):
        arrived(glog.at[part_of(1 - core, m)], go_r.at[m])

    for k in range(chunks):

        @pl.when(z < last)
        def _():
            sent(bb[k].at[block(z)], ou_s.at[k])

        @pl.when(z > 0)
        def _():
            sent(bb[k].at[block(z)], od_s.at[k])

        for at in range(1, last):

            @pl.when(z == at)
            def _():
                sent(bb[k].at[pl.ds(0, at * cb)], fu_s.at[k])
                sent(bb[k].at[pl.ds((at + 1) * cb, (last - at) * cb)], fd_s.at[k])

    for k in range(turns):
        for at in range(lines):

            @pl.when(z == at)
            def _():
                if at < last:
                    sent(es[k].at[pl.ds((at + 1) * cb, (last - at) * cb)], ru_s.at[k])
                if at > 0:
                    sent(es[k].at[pl.ds(0, at * cb)], rd_s.at[k])

    three = pl.ds(0, len(mates))
    sent(ab.at[three, half(0)], a_s)
    sent(ab.at[three, half(0)], a2_s)
    sent(rs.at[three], r_s)
    for k in range(chunks):
        sent(cr[k].at[three], c_s.at[k])
    sent(s1.at[three], s1_s)
    sent(s2.at[pl.ds(0, last)], s2_s)
    sent(ss.at[0], ss_s)
    for k in range(turns):
        sent(ds[k].at[pl.ds(0, len(mates) * rows)], d_s.at[k])
    sent(inn.at[0], in_s)
    sent(l1.at[three], l1_s)
    sent(l2.at[pl.ds(0, last)], l2_s)
    sent(fr.at[three], f_s)
    sent(fx, fx_s)
    sent(glog.at[half(0)], go_s)


def lane_groups(value):
    parts = [value[:, at : at + LANES] for at in range(0, value.shape[1], LANES)]
    return functools.reduce(lambda a, b: a + b, parts)


def grouped(refs, sizes):
    at = 0
    for size in sizes:
        yield refs[at : at + size]
        at += size


def deliver(pred_in, loss_in, glog_in, gexp_in, pred_ref, loss_ref, glog_ref, gexp_ref, sems):
    slides, slide_rows = pred_ref.shape[0], pred_ref.shape[1]
    copies = [pltpu.make_async_copy(gexp_in, gexp_ref, sems.at[2 * slides])]
    for m in range(slides):
        part = pl.ds(m * slide_rows, slide_rows)
        copies.append(pltpu.make_async_copy(glog_in.at[part], glog_ref.at[m], sems.at[m]))
        copies.append(pltpu.make_async_copy(pred_in.at[part], pred_ref.at[m], sems.at[slides + m]))
    for copy in copies:
        copy.start()
    loss_ref[...] = loss_in[...]
    for copy in copies:
        copy.wait()


def plane_call(logits, expr, spatial, slide_spots, spot_cells, cell_prior, lines):
    slides, slide_rows, cells = logits.shape
    rows = slides * slide_rows
    cb, genes = expr.shape
    quarter = lines * cb
    spots = PLANE * rows
    chunks, turns = len(FORWARD), len(BACKWARD)
    dma = pltpu.SemaphoreType.DMA
    vmem = pltpu.VMEM
    anywhere = pl.BlockSpec(memory_space=pl.ANY)
    in_vmem = pl.BlockSpec(memory_space=pltpu.VMEM)
    scratch = [
        pltpu.SMEM((slides,), jnp.int32),
        vmem((slides, slide_rows), jnp.int32),
        vmem((1, cells), jnp.int32),
        vmem((rows, cells), F32),
        vmem((PLANE, slide_rows, quarter), F32),
        vmem((rows, genes), F32),
        vmem((cb, genes), F32),
        vmem((PLANE, rows, quarter), F32),
        vmem((PLANE, rows, quarter), F32),
        vmem((PLANE, rows, quarter), F32),
        vmem((spots, quarter), BF16),
        vmem((spots, quarter), BF16),
        vmem((quarter, spots), BF16),
        vmem((quarter, spots), BF16),
        vmem((quarter, genes), BF16),
        vmem((quarter, genes), BF16),
        vmem((3, rows, LANES), F32),
        vmem((PLANE, 8, genes), F32),
        vmem((lines, 8, genes), F32),
        vmem((8, genes), F32),
        vmem((2, rows, LANES), F32),
        vmem((3, rows, LANES), F32),
        vmem((PLANE, 8, rows), F32),
        vmem((spots, genes), BF16),
        vmem((spots, genes), BF16),
        vmem((spots, quarter), F32),
        vmem((PLANE, slide_rows, quarter), F32),
        vmem((PLANE, slide_rows, quarter), F32),
        vmem((PLANE, slide_rows, quarter), F32),
        vmem((PLANE, slide_rows, quarter), F32),
        vmem((2, rows, LANES), F32),
        vmem((PLANE, 8, LANES), F32),
        vmem((lines, 8, LANES), F32),
        dma((2 * slides + 4,)),
        dma((chunks,)),
        dma((chunks,)),
        dma((chunks,)),
        dma((chunks,)),
        dma((chunks,)),
        dma((chunks,)),
        dma((chunks,)),
        dma((chunks,)),
        dma,
        dma((PLANE,)),
        dma,
        dma((PLANE,)),
        dma,
        dma((PLANE,)),
        dma((chunks,)),
        dma((chunks, PLANE)),
        dma,
        dma((2, PLANE)),
        dma,
        dma((2, lines)),
        dma,
        dma,
        dma((turns,)),
        dma((turns, PLANE)),
        dma((turns,)),
        dma((turns, lines)),
        dma((turns,)),
        dma((turns, lines)),
        dma,
        dma((PLANE,)),
        dma,
        dma((PLANE,)),
        dma,
        dma((2,)),
        dma,
        dma,
        dma,
        dma((PLANE,)),
        dma,
        dma((lines,)),
    ]
    for shape, widths in (
        ((quarter,), FORWARD),
        ((spots,), FORWARD),
        ((PLANE, rows), FORWARD),
        ((spots,), BACKWARD),
        ((quarter,), BACKWARD),
        ((quarter,), BACKWARD),
        ((quarter,), BACKWARD),
    ):
        scratch += [vmem(shape + (width,), F32) for width in widths]
    in_hbm = functools.partial(pltpu.with_memory_space_constraint, memory_space=pltpu.HBM)
    in_place = functools.partial(pltpu.with_memory_space_constraint, memory_space=pltpu.VMEM)
    results = pl.pallas_call(
        functools.partial(plane_kernel, lines, FORWARD, BACKWARD),
        out_shape=(
            vmem((rows, genes), F32),
            jax.ShapeDtypeStruct((1, 1), F32),
            vmem((rows, cells), F32),
            vmem((cb, genes), F32),
        ),
        in_specs=[anywhere] * 6,
        out_specs=(in_vmem,) * 4,
        scratch_shapes=scratch,
        compiler_params=pltpu.CompilerParams(
            collective_id=0, has_side_effects=True, vmem_limit_bytes=48 * 1024 * 1024
        ),
    )(*map(in_hbm, (logits, expr, spatial, slide_spots, spot_cells, cell_prior.reshape(1, cells))))
    pred, loss, grad_logits, grad_expr = pl.pallas_call(
        deliver,
        out_shape=(
            jax.ShapeDtypeStruct((slides, slide_rows, genes), F32),
            jax.ShapeDtypeStruct((1, 1), F32),
            jax.ShapeDtypeStruct((slides, slide_rows, cells), F32),
            jax.ShapeDtypeStruct((cb, genes), F32),
        ),
        in_specs=[anywhere, in_vmem, anywhere, anywhere],
        out_specs=(anywhere, in_vmem, anywhere, anywhere),
        scratch_shapes=[dma((2 * slides + 1,))],
        compiler_params=pltpu.CompilerParams(vmem_limit_bytes=4 * 1024 * 1024),
    )(in_place(results[0]), results[1], in_place(results[2]), in_place(results[3]))
    return pred, loss.reshape(()), grad_logits, grad_expr


def general_plan(logits, expr, spatial, slide_spots, spot_cells, cell_prior):
    place = lax.axis_index("spot")
    side = lax.axis_index("gene")
    rows_all = logits.shape[1]
    cell_rows = expr.shape[0]
    weights = cell_prior.astype(jnp.float32) / fixed_point
    gene_share = (place == 0).astype(jnp.float32)
    row_share = (side == 0).astype(jnp.float32)
    own_weights = lax.dynamic_slice_in_dim(weights, place * cell_rows, cell_rows, 0)
    expr_acc = jnp.zeros((cell_rows, expr.shape[1]), jnp.float32)
    loss_local = jnp.zeros((), jnp.float32)
    pred_list = []
    grad_list = []
    for slide in range(logits.shape[0]):
        logit_rows = logits[slide]
        counted = spot_cells[slide].astype(jnp.float32)
        target = spatial[slide]
        positions = place * rows_all + jnp.arange(rows_all, dtype=jnp.int32)
        valid = (positions < slide_spots[slide]).astype(jnp.float32)
        peak = jnp.max(logit_rows, axis=1, keepdims=True)
        raised = jnp.exp(logit_rows - peak)
        probs = raised / jnp.sum(raised, axis=1, keepdims=True)
        mass = jnp.dot(probs, weights, precision=lax.Precision.HIGHEST)
        blocks = lax.all_to_all(probs, "spot", split_axis=1, concat_axis=0, tiled=True)
        pred = lax.psum_scatter(
            jnp.dot(blocks, expr, precision=lax.Precision.HIGHEST),
            "spot",
            scatter_dimension=0,
            tiled=True,
        )
        gene_dot = jnp.sum(valid[:, None] * pred * target, axis=0)
        gene_pred = jnp.sum(valid[:, None] * pred * pred, axis=0)
        gene_true = jnp.sum(valid[:, None] * target * target, axis=0)
        mass_part = jnp.sum(valid * mass)
        kcell = valid * counted
        cell_part = jnp.sum(kcell)
        spot_dot = jnp.sum(pred * target, axis=1)
        spot_pred = jnp.sum(pred * pred, axis=1)
        spot_true = jnp.sum(target * target, axis=1)
        gene_dot, gene_pred, gene_true, mass_total, cell_total = lax.psum(
            (gene_dot, gene_pred, gene_true, mass_part, cell_part), "spot"
        )
        spot_dot, spot_pred, spot_true = lax.psum((spot_dot, spot_pred, spot_true), "gene")
        gene_inv = lax.rsqrt(gene_pred * gene_true + tiny)
        cos_gene = gene_dot * gene_inv
        spot_inv = lax.rsqrt(spot_pred * spot_true + tiny)
        cos_spot = spot_dot * spot_inv
        share = kcell / cell_total
        scale_count = slide_spots[slide].astype(jnp.float32)
        kl_part = jnp.sum(
            share * (jnp.log(counted) - jnp.log(cell_total) - jnp.log(mass) + jnp.log(mass_total))
        )
        loss_local = loss_local - gene_share * jnp.sum(cos_gene)
        loss_local = loss_local + row_share * (scale_count * kl_part - jnp.sum(valid * cos_spot))
        gene_back = cos_gene * gene_true / (gene_pred * gene_true + tiny)
        spot_back = cos_spot * spot_true / (spot_pred * spot_true + tiny)
        dpred = -valid[:, None] * (
            target * (gene_inv[None, :] + spot_inv[:, None])
            - pred * gene_back[None, :]
            - pred * spot_back[:, None]
        )
        dmass = scale_count * valid * (1.0 / mass_total - share / mass)
        pred_list.append(pred)
        grads_full, mass_full = (
            lax.all_gather(dpred, "spot", axis=0, tiled=True),
            lax.all_gather(dmass, "spot", axis=0, tiled=True),
        )
        dprob_cells = jnp.dot(grads_full, expr.T, precision=lax.Precision.HIGHEST)
        dprob_cells = lax.psum(dprob_cells, "gene")
        expr_acc = expr_acc + lax.dot_general(
            blocks, grads_full, (((0,), (0,)), ((), ())), precision=lax.Precision.HIGHEST
        )
        dprob_cells = dprob_cells + mass_full[:, None] * own_weights[None, :]
        dprob_rows = lax.all_to_all(dprob_cells, "spot", split_axis=0, concat_axis=1, tiled=True)
        inner = jnp.sum(probs * dprob_rows, axis=1, keepdims=True)
        dlogit = probs * (dprob_rows - inner)
        grad_list.append(dlogit)
    loss = lax.psum(loss_local, ("spot", "gene"))
    return (jnp.stack(pred_list), loss, jnp.stack(grad_list), expr_acc)


def solution(mesh):
    places = mesh.shape["spot"]

    def on_device(logits, expr, spatial, slide_spots, spot_cells, cell_prior):
        if places == PLANE * PLANE and mesh.shape["gene"] == 2 and expr.shape[1] == sum(FORWARD):
            return plane_call(
                logits, expr, spatial, slide_spots, spot_cells, cell_prior, places // PLANE
            )
        return general_plan(logits, expr, spatial, slide_spots, spot_cells, cell_prior)

    in_specs = (
        P(None, "spot", None),
        P("spot", "gene"),
        P(None, "spot", "gene"),
        P(),
        P(None, "spot"),
        P(),
    )
    out_specs = (P(None, "spot", "gene"), P(), P(None, "spot", None), P("spot", "gene"))
    return jax.shard_map(
        on_device, mesh=mesh, in_specs=in_specs, out_specs=out_specs, check_vma=False
    )
```

```python
import functools

import jax
import jax.numpy as jnp
from jax import lax
from jax.experimental import pallas as pl
from jax.experimental.pallas import tpu as pltpu
from jax.sharding import PartitionSpec as P

tiny = 1e-06
fixed_point = 16384.0
F32 = jnp.float32
BF16 = jnp.bfloat16
MESH = pl.DeviceIdType.MESH

PLANE = 4
LANES = 128
STEP_ROWS = 16
FORWARD = (256, 256, 256, 128, 128)
BACKWARD = (128, 128, 256, 256, 256)
SPLIT = 2
LEAD = 2
EARLY = 3
STEPS = (
    ("far", 0),
    ("share",),
    ("near", 0),
    ("far", 1),
    ("take",),
    ("whole", 0),
    ("product", 0),
    ("near", 1),
    ("far", 2),
    ("whole", 1),
    ("product", 1),
    ("far", 3),
    ("near", 2),
    ("whole", 2),
    ("far", 4),
    ("product", 2),
    ("turn", 0),
    ("near", 3),
    ("sum", 0),
    ("whole", 3),
    ("near", 4),
    ("sum", 1),
    ("product", 3),
    ("whole", 4),
    ("sum", 2),
    ("plane", 0),
    ("product", 4),
    ("turn", 1),
    ("sum", 3),
    ("line", 0),
    ("sum", 4),
    ("plane", 1),
    ("cores",),
    ("genes", 0),
    ("spots",),
    ("grad", 0),
    ("grad", 1),
    ("grad", 2),
    ("backward", 0),
    ("line", 1),
    ("grad", 3),
    ("probs", 0),
    ("backward", 1),
    ("add_near", 0),
    ("backward", 2),
    ("genes", 1),
    ("probs", 1),
    ("grad", 4),
    ("probs", 2),
    ("add_far", 0),
    ("expr", 0),
    ("backward", 3),
    ("probs", 3),
    ("add_near", 1),
    ("backward", 4),
    ("probs", 4),
    ("exchange",),
    ("terms",),
    ("add_near", 2),
    ("return",),
    ("add_near", 3),
    ("add_far", 1),
    ("add_far", 2),
    ("expr", 1),
    ("expr", 2),
    ("add_far", 3),
    ("loss",),
    ("logits",),
    ("add_near", 4),
    ("expr", 3),
    ("add_far", 4),
    ("expr", 4),
)


def halves(value):
    high = value.astype(BF16)
    return high, (value - high.astype(F32)).astype(BF16)


def product(a_high, a_low, b_high, b_low, contract):
    def one(a, b):
        return lax.dot_general(a, b, (contract, ((), ())), preferred_element_type=F32)

    return one(a_high, b_high) + (one(a_high, b_low) + one(a_low, b_high))


def plane_kernel(lines, forward_widths, backward_widths, *refs):
    chunks, turns = len(forward_widths), len(backward_widths)
    (
        (logits_ref, expr_ref, spatial_ref, count_in, cells_in, prior_in),
        (pr, loss_ref, glog, ge),
        (count_ref, cells_ref, prior_ref, lg, lq, tg, ex, pq, ab, af, ahi, alo, thi, tlo, bhi, blo, sacc, s1, s2, gv, ss, rowv, rs),
        (dhi, dlo, fs, fx, fy, fz, fr, inn, l1, l2),
        (loc, ou_s, ou_r, od_s, od_r, fu_s, fu_r, fd_s, fd_r, a_s, a_r, a2_s, a2_r, r_s, r_r),
        (c_s, c_r, s1_s, s1_r, s2_s, s2_r, ss_s, ss_r, d_s, d_r, ru_s, ru_r, rd_s, rd_r),
        (f_s, f_r, fx_s, fx_r, go_s, go_r, in_s, in_r, l1_s, l1_r, l2_s, l2_r),
        bb,
        cs,
        cr,
        ds,
        es,
        ru,
        rd,
    ) = grouped(refs, (6, 4, 23, 10, 15, 14, 12, chunks, chunks, chunks, turns, turns, turns, turns))
    place = lax.axis_index("spot")
    core = lax.axis_index("gene")
    z = place // PLANE
    q = place % PLANE
    col, row = q % 2, q // 2
    mates = ((1 - row) * 2 + 1 - col, row * 2 + 1 - col, (1 - row) * 2 + col)
    others = tuple((z + step) % lines for step in range(1, lines))
    up, down = (place + PLANE, core), (place - PLANE, core)
    sibling = (place, 1 - core)
    slides, slide_rows = logits_ref.shape[0], logits_ref.shape[1]
    rows = slides * slide_rows
    cb = expr_ref.shape[0]
    genes = expr_ref.shape[1]
    last = lines - 1

    def mate(p):
        return (z * PLANE + p, core)

    def send(src, dst, send_sem, recv_sem, device):
        copy = pltpu.make_async_remote_copy(
            src_ref=src, dst_ref=dst, send_sem=send_sem, recv_sem=recv_sem, device_id=device, device_id_type=MESH
        )
        copy.start()

    def arrived(dst, recv_sem):
        pltpu.make_async_copy(dst, dst, recv_sem).wait()

    sent = arrived

    def cols(k):
        return pl.ds(sum(forward_widths[:k]), forward_widths[k])

    def turn_cols(k):
        return pl.ds(sum(backward_widths[:k]), backward_widths[k])

    def block(index):
        return pl.ds(pl.multiple_of(index * cb, cb), cb)

    def share(index):
        return pl.ds(pl.multiple_of(index * rows, rows), rows)

    def half(index):
        return pl.ds(pl.multiple_of(index * slide_rows, slide_rows), slide_rows)

    small = ((prior_in, prior_ref), (count_in, count_ref), (cells_in, cells_ref))
    pltpu.make_async_copy(expr_ref, ex, loc.at[2 * slides]).start()
    for m in range(slides):
        pltpu.make_async_copy(logits_ref.at[m], lg.at[half(m)], loc.at[m]).start()
    for at, (src, dst) in enumerate(small):
        pltpu.make_async_copy(src, dst, loc.at[2 * slides + 1 + at]).start()
    for m in range(slides):
        pltpu.make_async_copy(spatial_ref.at[m], tg.at[half(m)], loc.at[slides + m]).start()

    barrier = pltpu.get_barrier_semaphore()
    for p in mates:
        pl.semaphore_signal(barrier, inc=1, device_id=mate(p), device_id_type=MESH)
    for o in others:
        pl.semaphore_signal(barrier, inc=1, device_id=(o * PLANE + q, core), device_id_type=MESH)
    pl.semaphore_signal(barrier, inc=1, device_id=sibling, device_id_type=MESH)
    pltpu.make_async_copy(expr_ref, ex, loc.at[2 * slides]).wait()
    for k in range(chunks):
        bb[k][block(z), :] = ex[:, cols(k)]
    for m in range(slides):
        pltpu.make_async_copy(logits_ref.at[m], lg.at[half(m)], loc.at[m]).wait()
    for p in range(PLANE):
        for line in range(lines):
            lq[p, :, pl.ds(line * cb, cb)] = lg[half(core), pl.ds((line * PLANE + p) * cb, cb)]
    pl.semaphore_wait(barrier, len(mates) + len(others) + 1)

    def own_up(k):
        here = bb[k].at[block(z)]
        send(here, here, ou_s.at[k], ou_r.at[k], up)

    def own_down(k):
        here = bb[k].at[block(z)]
        send(here, here, od_s.at[k], od_r.at[k], down)

    def low(at):
        return 2 * at < lines

    for at in range(lines):

        @pl.when(z == at)
        def _():
            for k in range(chunks):
                if at < last and (not low(at) or at == 0 or k < LEAD):
                    own_up(k)
                if at > 0 and (low(at) or at == last or k < LEAD):
                    own_down(k)

    for p in mates:
        send(lq.at[p], ab.at[q, half(core)], a_s, a_r.at[q], mate(p))

    def from_below(k, at):
        arrived(bb[k].at[pl.ds((at - 1) * cb, cb)], ou_r.at[k])
        if at > 1:
            arrived(bb[k].at[pl.ds(0, (at - 1) * cb)], fu_r.at[k])

    def from_above(k, at):
        arrived(bb[k].at[pl.ds((at + 1) * cb, cb)], od_r.at[k])
        if at < last - 1:
            arrived(bb[k].at[pl.ds((at + 2) * cb, (last - 1 - at) * cb)], fd_r.at[k])

    def upward(k, at):
        from_below(k, at)
        here = bb[k].at[pl.ds(0, at * cb)]
        send(here, here, fu_s.at[k], fu_r.at[k], up)

    def downward(k, at):
        from_above(k, at)
        here = bb[k].at[pl.ds((at + 1) * cb, (last - at) * cb)]
        send(here, here, fd_s.at[k], fd_r.at[k], down)

    def forward_far(k):
        for at in range(1, last):

            @pl.when(z == at)
            def _():
                (upward if low(at) else downward)(k, at)
                if k + LEAD < chunks:
                    (own_up if low(at) else own_down)(k + LEAD)

    def forward_near(k):
        for at in range(1, last):

            @pl.when(z == at)
            def _():
                (downward if low(at) else upward)(k, at)

    def gathered(k):
        @pl.when(z == 0)
        def _():
            from_above(k, 0)

        @pl.when(z == last)
        def _():
            from_below(k, last)

    for at, (src, dst) in enumerate(small):
        pltpu.make_async_copy(src, dst, loc.at[2 * slides + 1 + at]).wait()
    weights = prior_ref[...].astype(F32) / fixed_point

    @pl.loop(0, rows // STEP_ROWS)
    def _(step):
        at = pl.ds(pl.multiple_of(step * STEP_ROWS, STEP_ROWS), STEP_ROWS)
        value = lg[at, :]
        peak = jnp.max(value, axis=1, keepdims=True)
        raised = jnp.exp(value - peak)
        scale = 1.0 / jnp.sum(raised, axis=1, keepdims=True)
        probs = raised * scale
        mass_rows = jnp.sum(probs * weights, axis=1, keepdims=True)
        rowv[0, at, :] = jnp.broadcast_to(mass_rows, (STEP_ROWS, LANES))
        rowv[1, at, :] = jnp.broadcast_to(peak, (STEP_ROWS, LANES))
        rowv[2, at, :] = jnp.broadcast_to(scale, (STEP_ROWS, LANES))
        for p in range(PLANE):
            for line in range(lines):
                at_cells = (line * PLANE + p) * cb
                pq[p, at, pl.ds(line * cb, cb)] = probs[:, at_cells : at_cells + cb]

    wide = lax.broadcasted_iota(jnp.int32, (rows, LANES), 1)
    rs[q] = jnp.where(wide == 0, rowv[1], rowv[2]).T[0:8]
    for p in mates:
        send(rs.at[q], rs.at[q], r_s, r_r.at[q], mate(p))

    rid = lax.broadcasted_iota(jnp.int32, (rows, 1), 0)
    first = rid < slide_rows
    position = place * slide_rows + jnp.where(first, rid, rid - slide_rows)
    count = jnp.where(first, count_ref[0], count_ref[1])
    valid = (position < count).astype(F32)
    scale_count = count.astype(F32)
    square = (slide_rows, slide_rows)
    eye = lax.broadcasted_iota(jnp.int32, square, 0) == lax.broadcasted_iota(jnp.int32, square, 1)
    counted = jnp.concatenate(
        [
            jnp.sum(jnp.where(eye, cells_ref[m : m + 1, :].astype(F32), 0.0), axis=1, keepdims=True)
            for m in range(slides)
        ],
        axis=0,
    )
    mass = rowv[0, :, 0:1]
    kcell = valid * counted

    def by_slide(value):
        return [jnp.sum(value[m * slide_rows : (m + 1) * slide_rows], axis=0, keepdims=True) for m in range(slides)]

    mass_parts = by_slide(valid * mass)
    cell_parts = by_slide(kcell)
    lane = lax.broadcasted_iota(jnp.int32, (1, LANES), 1)
    scalars = jnp.zeros((1, LANES), F32)
    for at, value in enumerate(mass_parts + cell_parts):
        scalars = jnp.where(lane == at, value, scalars)
    for m in range(slides):
        pltpu.make_async_copy(spatial_ref.at[m], tg.at[half(m)], loc.at[slides + m]).wait()
    sacc[...] = jnp.zeros_like(sacc)
    s1[q, 3 * slides :, :] = jnp.zeros((8 - 3 * slides, genes), F32)
    s1[q, 3 * slides : 3 * slides + 1, 0:LANES] = scalars

    def share_logits():
        for p in (mates[1], mates[2], mates[0]):
            here = ab.at[p, half(core)]
            arrived(here, a_r.at[p])
            send(here, here, a2_s, a2_r.at[p], sibling)

    def take_probs():
        af[q] = pq[q]
        ahi[share(q), :], alo[share(q), :] = halves(pq[q])
        for p in (mates[1], mates[2], mates[0]):
            arrived(rs.at[p], r_r.at[p])
            arrived(ab.at[p, half(1 - core)], a2_r.at[p])
            by_row = rs[p].T
            probs = jnp.exp(ab[p] - by_row[:, 0:1]) * by_row[:, 1:2]
            af[p] = probs
            ahi[share(p), :], alo[share(p), :] = halves(probs)

    def transpose(part):
        for p in (2 * part, 2 * part + 1):
            high, low_part = halves(af[p].T)
            thi[:, share(p)], tlo[:, share(p)] = high, low_part

    def forward_product(k):
        high, low = halves(bb[k][...])
        bhi[:, cols(k)], blo[:, cols(k)] = high, low
        if k < chunks - 1:
            cs[k][...] = product(ahi[...], alo[...], high, low, ((1,), (0,)))
            for p in mates:
                pass_pred(k, p)
        else:
            for side, served in ((1 - row, (mates[0], mates[2])), (row, (mates[1],))):
                pair = pl.ds(pl.multiple_of(2 * side * rows, 2 * rows), 2 * rows)
                cs[k][pair, :] = product(ahi[pair, :], alo[pair, :], high, low, ((1,), (0,)))
                for p in served:
                    pass_pred(k, p)

    def pass_pred(k, p):
        send(cs[k].at[share(p)], cr[k].at[q], c_s.at[k], c_r.at[k, q], mate(p))

    def finish_pred(k):
        total = cs[k][share(q), :]
        for p in mates:
            arrived(cr[k].at[p], c_r.at[k, p])
            total = total + cr[k][p]
        pr[:, cols(k)] = total
        truth = tg[:, cols(k)]
        for at, value in enumerate((total * truth, total * total, truth * truth)):
            sacc[at] += lane_groups(value)
        kept = valid * total
        stats = by_slide(kept * truth) + by_slide(kept * total) + by_slide(valid * truth * truth)
        s1[q, 0 : 3 * slides, cols(k)] = jnp.concatenate(stats, axis=0)

    early = sum(forward_widths[:EARLY])
    parts = (pl.ds(0, early), pl.ds(early, genes - early))

    def sum_plane(at):
        for p in mates:
            send(s1.at[q, :, parts[at]], s1.at[q, :, parts[at]], s1_s, s1_r.at[at, q], mate(p))

    def sum_line(at):
        for p in mates:
            arrived(s1.at[p, :, parts[at]], s1_r.at[at, p])
        s2[z, :, parts[at]] = (s1[0, :, parts[at]] + s1[1, :, parts[at]]) + (s1[2, :, parts[at]] + s1[3, :, parts[at]])
        for o in others:
            send(s2.at[z, :, parts[at]], s2.at[z, :, parts[at]], s2_s, s2_r.at[at, z], (o * PLANE + q, core))

    kept = {}

    def finish_genes(at):
        for o in others:
            arrived(s2.at[o, :, parts[at]], s2_r.at[at, o])
        total = s2[0, :, parts[at]]
        for line in range(1, lines):
            total = total + s2[line, :, parts[at]]
        gene_dot, gene_pred, gene_true = total[0:2], total[2:4], total[4:6]
        gene_inv = lax.rsqrt(gene_pred * gene_true + tiny)
        cos_gene = gene_dot * gene_inv
        gv[0:2, parts[at]] = gene_inv
        gv[2:4, parts[at]] = cos_gene * gene_true / (gene_pred * gene_true + tiny)
        kept["genes", at] = jnp.sum(jnp.sum(cos_gene, axis=1, keepdims=True), axis=0, keepdims=True)
        if at == 0:
            kept["mass"] = jnp.where(first, total[6:7, 0:1], total[6:7, 1:2])
            kept["cells"] = jnp.where(first, total[6:7, 2:3], total[6:7, 3:4])

    def sum_cores():
        sums = [jnp.sum(sacc[at], axis=1, keepdims=True) for at in range(3)]
        ss[core] = jnp.where(wide == 0, sums[0], jnp.where(wide == 1, sums[1], sums[2]))
        send(ss.at[core], ss.at[core], ss_s, ss_r, sibling)

    def finish_spots():
        arrived(ss.at[1 - core], ss_r)
        spot = ss[0] + ss[1]
        spot_dot, spot_pred, spot_true = spot[:, 0:1], spot[:, 1:2], spot[:, 2:3]
        spot_inv = lax.rsqrt(spot_pred * spot_true + tiny)
        cos_spot = spot_dot * spot_inv
        kept["inverse"], kept["cos"] = spot_inv, cos_spot
        kept["back"] = cos_spot * spot_true / (spot_pred * spot_true + tiny)
        sacc[0] = jnp.zeros_like(sacc[0])

    def send_grad(k):
        spot_inv, spot_back = kept["inverse"], kept["back"]
        pieces = []
        for m in range(slides):
            lo, hi = m * slide_rows, (m + 1) * slide_rows
            truth, guess = tg[lo:hi, turn_cols(k)], pr[lo:hi, turn_cols(k)]
            inverse, back = gv[m : m + 1, turn_cols(k)], gv[2 + m : 3 + m, turn_cols(k)]
            pieces.append(
                -valid[lo:hi]
                * (truth * (inverse + spot_inv[lo:hi]) - guess * back - guess * spot_back[lo:hi])
            )
        grad = jnp.concatenate(pieces, axis=0)
        here = ds[k].at[share(q)]
        here[...] = grad
        for p in mates:
            send(here, here, d_s.at[k], d_r.at[k, q], mate(p))
        sacc[0] += lane_groups(grad * pr[:, turn_cols(k)])

    def send_terms():
        mass_total, cell_total = kept["mass"], kept["cells"]
        portion = kcell / cell_total
        kl_rows = portion * (jnp.log(counted) - jnp.log(cell_total) - jnp.log(mass) + jnp.log(mass_total))
        dmass = scale_count * valid * (1.0 / mass_total - portion / mass)
        terms = jnp.sum(scale_count * kl_rows - valid * kept["cos"], axis=0, keepdims=True)
        l1[q] = jnp.broadcast_to(terms, (8, LANES))
        for p in mates:
            send(l1.at[q], l1.at[q], l1_s, l1_r.at[q], mate(p))
        inner = jnp.sum(sacc[0], axis=1, keepdims=True)
        inn[core] = jnp.where(wide == 0, inner, kept["genes", 0] + kept["genes", 1])
        send(inn.at[core], inn.at[core], in_s, in_r, sibling)
        rowv[1] = jnp.broadcast_to(dmass, (rows, LANES))

    middle = lines // 2

    def backward_product(k):
        for p in mates:
            arrived(ds[k].at[share(p)], d_r.at[k, p])
        high, low_part = halves(ds[k][...])
        dhi[:, turn_cols(k)], dlo[:, turn_cols(k)] = high, low_part
        if not halved(k):
            es[k][...] = product(thi[...], tlo[...], high, low_part, ((1,), (0,)))

        for turn in range(2):
            if halved(k):
                side = (1 - z // middle) if turn == 0 else z // middle
                pair = pl.ds(pl.multiple_of(side * middle * cb, middle * cb), middle * cb)
                es[k][pair, :] = product(thi[pair, :], tlo[pair, :], high, low_part, ((1,), (0,)))

            @pl.when(z == 0)
            def _():
                if halved(k):
                    pass_up(k, middle if turn == 0 else 1, middle if turn == 0 else middle - 1, turn)
                elif whole(k):
                    if turn == 0:
                        pass_up(k, 1, last, 0)
                elif turn == 0:
                    for line in range(last, 0, -1):
                        pass_up(k, line, 1, line)

            @pl.when(z == last)
            def _():
                if halved(k):
                    pass_down(k, 0 if turn == 0 else middle, middle if turn == 0 else middle - 1, turn)
                elif whole(k):
                    if turn == 0:
                        pass_down(k, 0, last, 0)
                elif turn == 0:
                    for line in range(last):
                        pass_down(k, line, 1, line)

    def halved(k):
        return k == 0

    def whole(k):
        return 0 < k < turns - SPLIT

    def pass_up(k, line, count, slot):
        here = pl.ds(line * cb, count * cb)
        send(es[k].at[here], ru[k].at[here], ru_s.at[k], ru_r.at[k, slot], up)

    def pass_down(k, line, count, slot):
        here = pl.ds(line * cb, count * cb)
        send(es[k].at[here], rd[k].at[here], rd_s.at[k], rd_r.at[k, slot], down)

    def take_up(k, line, count, slot):
        arrived(ru[k].at[pl.ds(line * cb, count * cb)], ru_r.at[k, slot])

    def take_down(k, line, count, slot):
        arrived(rd[k].at[pl.ds(line * cb, count * cb)], rd_r.at[k, slot])

    def add_up(k, line, count):
        here = pl.ds(line * cb, count * cb)
        es[k][here, :] += ru[k][here, :]

    def add_down(k, line, count):
        here = pl.ds(line * cb, count * cb)
        es[k][here, :] += rd[k][here, :]

    def rising(k, at):
        if halved(k) or whole(k):
            start = middle if halved(k) else at
            take_up(k, start, lines - start, 0)
            above = max(at + 1, start)
            add_up(k, above, lines - above)
            pass_up(k, above, lines - above, 0)
        else:
            for line in range(last, at, -1):
                take_up(k, line, 1, line)
                add_up(k, line, 1)
                pass_up(k, line, 1, line)

    def falling(k, at):
        if halved(k) or whole(k):
            end = middle if halved(k) else at + 1
            take_down(k, 0, end, 0)
            below = min(at, end)
            add_down(k, 0, below)
            pass_down(k, 0, below, 0)
        else:
            for line in range(at):
                take_down(k, line, 1, line)
                add_down(k, line, 1)
                pass_down(k, line, 1, line)

    def add_near(k):
        for at in range(1, last):

            @pl.when(z == at)
            def _():
                (rising if low(at) else falling)(k, at)

    def add_far(k):
        for at in range(1, last):

            @pl.when(z == at)
            def _():
                (falling if low(at) else rising)(k, at)

    def finish_expr(k):
        for at in range(lines):

            @pl.when(z == at)
            def _():
                own = pl.ds(at * cb, cb)
                total = es[k][own, :]
                if at > 0:
                    if halved(k) and at < middle:
                        take_up(k, at, 1, 1)
                    elif at == last and (halved(k) or whole(k)):
                        take_up(k, at, 1, 0)
                    elif not halved(k) and not whole(k):
                        take_up(k, at, 1, at)
                    total = total + ru[k][own, :]
                if at < last:
                    if halved(k) and at >= middle:
                        take_down(k, at, 1, 1)
                    elif at == 0 and (halved(k) or whole(k)):
                        take_down(k, at, 1, 0)
                    elif not halved(k) and not whole(k):
                        take_down(k, at, 1, at)
                    total = total + rd[k][own, :]
                ge[:, turn_cols(k)] = total

    def probs_gradient(k):
        at = turn_cols(k)
        part = product(dhi[:, at], dlo[:, at], bhi[:, at], blo[:, at], ((1,), (1,)))
        if k == 0:
            fs[...] = part
        else:
            fs[...] += part

    def slide_of(p, m):
        return pl.ds(pl.multiple_of(p * rows + m * slide_rows, slide_rows), slide_rows)

    def sum_probs_cores():
        for p in mates + (q,):
            fx[p] = fs[slide_of(p, 1 - core), :]
            send(fx.at[p], fy.at[p], fx_s, fx_r.at[p], sibling)

    def return_probs():
        for p in mates + (q,):
            arrived(fy.at[p], fx_r.at[p])
            fz[p] = fs[slide_of(p, core), :] + fy[p]
        for p in mates:
            send(fz.at[p], fr.at[q], f_s, f_r.at[q], mate(p))
        fr[q] = fz[q]

    def pass_terms():
        for p in mates:
            arrived(l1.at[p], l1_r.at[p])
        l2[z] = (l1[0] + l1[1]) + (l1[2] + l1[3])
        for o in others:
            send(l2.at[z], l2.at[z], l2_s, l2_r.at[z], (o * PLANE + q, core))

    def part_of(slide, m):
        start = slide * slide_rows + m * (slide_rows // 2)
        return pl.ds(pl.multiple_of(start, slide_rows // 2), slide_rows // 2)

    def finish_logits():
        arrived(inn.at[1 - core], in_r)
        rowv[2] = (inn[0] + inn[1]) + rowv[1] * rowv[0]
        for p in mates:
            arrived(fr.at[p], f_r.at[p])
        for m in range(2):

            @pl.loop(0, slide_rows // STEP_ROWS // 2)
            def _(step):
                row_at = (m * (slide_rows // STEP_ROWS // 2) + step) * STEP_ROWS
                at = pl.ds(pl.multiple_of(row_at, STEP_ROWS), STEP_ROWS)
                whole_at = pl.ds(pl.multiple_of(core * slide_rows + row_at, STEP_ROWS), STEP_ROWS)
                by_mass, total_inner = rowv[1, whole_at, 0:1], rowv[2, whole_at, 0:1]
                for p in range(PLANE):
                    for line in range(lines):
                        here, there = pl.ds(line * cb, cb), (line * PLANE + p) * cb
                        grad = fr[p, at, here] + by_mass * weights[:, there : there + cb]
                        glog[whole_at, pl.ds(there, cb)] = pq[p, whole_at, here] * (grad - total_inner)

            here = part_of(core, m)
            send(glog.at[here], glog.at[here], go_s, go_r.at[m], sibling)

    steps = {
        "far": forward_far,
        "near": forward_near,
        "share": share_logits,
        "take": take_probs,
        "whole": gathered,
        "product": forward_product,
        "sum": finish_pred,
        "turn": transpose,
        "plane": sum_plane,
        "line": sum_line,
        "genes": finish_genes,
        "cores": sum_cores,
        "spots": finish_spots,
        "grad": send_grad,
        "terms": send_terms,
        "backward": backward_product,
        "probs": probs_gradient,
        "exchange": sum_probs_cores,
        "return": return_probs,
        "loss": pass_terms,
        "logits": finish_logits,
        "add_near": add_near,
        "add_far": add_far,
        "expr": finish_expr,
    }
    for name, *where in STEPS:
        steps[name](*where)

    for o in others:
        arrived(l2.at[o], l2_r.at[o])
    loss = l2[0]
    for line in range(1, lines):
        loss = loss + l2[line]
    loss_ref[...] = loss[0:1, 0:1] - (inn[0, 0:1, 1:2] + inn[1, 0:1, 1:2])
    for m in range(2):
        arrived(glog.at[part_of(1 - core, m)], go_r.at[m])

    for k in range(chunks):

        @pl.when(z < last)
        def _():
            sent(bb[k].at[block(z)], ou_s.at[k])

        @pl.when(z > 0)
        def _():
            sent(bb[k].at[block(z)], od_s.at[k])

        for at in range(1, last):

            @pl.when(z == at)
            def _():
                sent(bb[k].at[pl.ds(0, at * cb)], fu_s.at[k])
                sent(bb[k].at[pl.ds((at + 1) * cb, (last - at) * cb)], fd_s.at[k])

    for k in range(turns):
        for at in range(lines):

            @pl.when(z == at)
            def _():
                if at < last:
                    sent(es[k].at[pl.ds((at + 1) * cb, (last - at) * cb)], ru_s.at[k])
                if at > 0:
                    sent(es[k].at[pl.ds(0, at * cb)], rd_s.at[k])

    three = pl.ds(0, len(mates))
    sent(ab.at[three, half(0)], a_s)
    sent(ab.at[three, half(0)], a2_s)
    sent(rs.at[three], r_s)
    for k in range(chunks):
        sent(cr[k].at[three], c_s.at[k])
    sent(s1.at[three], s1_s)
    sent(s2.at[pl.ds(0, last)], s2_s)
    sent(ss.at[0], ss_s)
    for k in range(turns):
        sent(ds[k].at[pl.ds(0, len(mates) * rows)], d_s.at[k])
    sent(inn.at[0], in_s)
    sent(l1.at[three], l1_s)
    sent(l2.at[pl.ds(0, last)], l2_s)
    sent(fr.at[three], f_s)
    sent(fx, fx_s)
    sent(glog.at[half(0)], go_s)


def lane_groups(value):
    parts = [value[:, at : at + LANES] for at in range(0, value.shape[1], LANES)]
    return functools.reduce(lambda a, b: a + b, parts)


def grouped(refs, sizes):
    at = 0
    for size in sizes:
        yield refs[at : at + size]
        at += size


def deliver(pred_in, loss_in, glog_in, gexp_in, pred_ref, loss_ref, glog_ref, gexp_ref, sems):
    slides, slide_rows = pred_ref.shape[0], pred_ref.shape[1]
    copies = []
    quarter = slide_rows // 4
    for at in range(4 * slides):
        part, where = pl.ds(at * quarter, quarter), pl.ds(at % 4 * quarter, quarter)
        copies.append(pltpu.make_async_copy(glog_in.at[part], glog_ref.at[at // 4, where], sems.at[0, at]))
        copies.append(pltpu.make_async_copy(pred_in.at[part], pred_ref.at[at // 4, where], sems.at[1, at]))
        copies.append(pltpu.make_async_copy(gexp_in.at[part], gexp_ref.at[part], sems.at[2, at]))
    for copy in copies:
        copy.start()
    loss_ref[...] = loss_in[...]
    for copy in copies:
        copy.wait()


def plane_call(logits, expr, spatial, slide_spots, spot_cells, cell_prior, lines):
    slides, slide_rows, cells = logits.shape
    rows = slides * slide_rows
    cb, genes = expr.shape
    quarter = lines * cb
    spots = PLANE * rows
    chunks, turns = len(FORWARD), len(BACKWARD)
    dma = pltpu.SemaphoreType.DMA
    vmem = pltpu.VMEM
    anywhere = pl.BlockSpec(memory_space=pl.ANY)
    in_vmem = pl.BlockSpec(memory_space=pltpu.VMEM)
    scratch = [
        pltpu.SMEM((slides,), jnp.int32),
        vmem((slides, slide_rows), jnp.int32),
        vmem((1, cells), jnp.int32),
        vmem((rows, cells), F32),
        vmem((PLANE, slide_rows, quarter), F32),
        vmem((rows, genes), F32),
        vmem((cb, genes), F32),
        vmem((PLANE, rows, quarter), F32),
        vmem((PLANE, rows, quarter), F32),
        vmem((PLANE, rows, quarter), F32),
        vmem((spots, quarter), BF16),
        vmem((spots, quarter), BF16),
        vmem((quarter, spots), BF16),
        vmem((quarter, spots), BF16),
        vmem((quarter, genes), BF16),
        vmem((quarter, genes), BF16),
        vmem((3, rows, LANES), F32),
        vmem((PLANE, 8, genes), F32),
        vmem((lines, 8, genes), F32),
        vmem((8, genes), F32),
        vmem((2, rows, LANES), F32),
        vmem((3, rows, LANES), F32),
        vmem((PLANE, 8, rows), F32),
        vmem((spots, genes), BF16),
        vmem((spots, genes), BF16),
        vmem((spots, quarter), F32),
        vmem((PLANE, slide_rows, quarter), F32),
        vmem((PLANE, slide_rows, quarter), F32),
        vmem((PLANE, slide_rows, quarter), F32),
        vmem((PLANE, slide_rows, quarter), F32),
        vmem((2, rows, LANES), F32),
        vmem((PLANE, 8, LANES), F32),
        vmem((lines, 8, LANES), F32),
        dma((2 * slides + 4,)),
        dma((chunks,)),
        dma((chunks,)),
        dma((chunks,)),
        dma((chunks,)),
        dma((chunks,)),
        dma((chunks,)),
        dma((chunks,)),
        dma((chunks,)),
        dma,
        dma((PLANE,)),
        dma,
        dma((PLANE,)),
        dma,
        dma((PLANE,)),
        dma((chunks,)),
        dma((chunks, PLANE)),
        dma,
        dma((2, PLANE)),
        dma,
        dma((2, lines)),
        dma,
        dma,
        dma((turns,)),
        dma((turns, PLANE)),
        dma((turns,)),
        dma((turns, lines)),
        dma((turns,)),
        dma((turns, lines)),
        dma,
        dma((PLANE,)),
        dma,
        dma((PLANE,)),
        dma,
        dma((2,)),
        dma,
        dma,
        dma,
        dma((PLANE,)),
        dma,
        dma((lines,)),
    ]
    for shape, widths in (
        ((quarter,), FORWARD),
        ((spots,), FORWARD),
        ((PLANE, rows), FORWARD),
        ((spots,), BACKWARD),
        ((quarter,), BACKWARD),
        ((quarter,), BACKWARD),
        ((quarter,), BACKWARD),
    ):
        scratch += [vmem(shape + (width,), F32) for width in widths]
    in_hbm = functools.partial(pltpu.with_memory_space_constraint, memory_space=pltpu.HBM)
    in_place = functools.partial(pltpu.with_memory_space_constraint, memory_space=pltpu.VMEM)
    results = pl.pallas_call(
        functools.partial(plane_kernel, lines, FORWARD, BACKWARD),
        out_shape=(
            vmem((rows, genes), F32),
            jax.ShapeDtypeStruct((1, 1), F32),
            vmem((rows, cells), F32),
            vmem((cb, genes), F32),
        ),
        in_specs=[anywhere] * 6,
        out_specs=(in_vmem,) * 4,
        scratch_shapes=scratch,
        compiler_params=pltpu.CompilerParams(
            collective_id=0, has_side_effects=True, vmem_limit_bytes=48 * 1024 * 1024
        ),
    )(*map(in_hbm, (logits, expr, spatial, slide_spots, spot_cells, cell_prior.reshape(1, cells))))
    pred, loss, grad_logits, grad_expr = pl.pallas_call(
        deliver,
        out_shape=(
            jax.ShapeDtypeStruct((slides, slide_rows, genes), F32),
            jax.ShapeDtypeStruct((1, 1), F32),
            jax.ShapeDtypeStruct((slides, slide_rows, cells), F32),
            jax.ShapeDtypeStruct((cb, genes), F32),
        ),
        in_specs=[anywhere, in_vmem, anywhere, anywhere],
        out_specs=(anywhere, in_vmem, anywhere, anywhere),
        scratch_shapes=[dma((3, 4 * slides))],
        compiler_params=pltpu.CompilerParams(vmem_limit_bytes=4 * 1024 * 1024),
    )(in_place(results[0]), results[1], in_place(results[2]), in_place(results[3]))
    return pred, loss.reshape(()), grad_logits, grad_expr


def general_plan(logits, expr, spatial, slide_spots, spot_cells, cell_prior):
    place = lax.axis_index("spot")
    side = lax.axis_index("gene")
    rows_all = logits.shape[1]
    cell_rows = expr.shape[0]
    weights = cell_prior.astype(jnp.float32) / fixed_point
    gene_share = (place == 0).astype(jnp.float32)
    row_share = (side == 0).astype(jnp.float32)
    own_weights = lax.dynamic_slice_in_dim(weights, place * cell_rows, cell_rows, 0)
    expr_acc = jnp.zeros((cell_rows, expr.shape[1]), jnp.float32)
    loss_local = jnp.zeros((), jnp.float32)
    pred_list = []
    grad_list = []
    for slide in range(logits.shape[0]):
        logit_rows = logits[slide]
        counted = spot_cells[slide].astype(jnp.float32)
        target = spatial[slide]
        positions = place * rows_all + jnp.arange(rows_all, dtype=jnp.int32)
        valid = (positions < slide_spots[slide]).astype(jnp.float32)
        peak = jnp.max(logit_rows, axis=1, keepdims=True)
        raised = jnp.exp(logit_rows - peak)
        probs = raised / jnp.sum(raised, axis=1, keepdims=True)
        mass = jnp.dot(probs, weights, precision=lax.Precision.HIGHEST)
        blocks = lax.all_to_all(probs, "spot", split_axis=1, concat_axis=0, tiled=True)
        pred = lax.psum_scatter(
            jnp.dot(blocks, expr, precision=lax.Precision.HIGHEST),
            "spot",
            scatter_dimension=0,
            tiled=True,
        )
        gene_dot = jnp.sum(valid[:, None] * pred * target, axis=0)
        gene_pred = jnp.sum(valid[:, None] * pred * pred, axis=0)
        gene_true = jnp.sum(valid[:, None] * target * target, axis=0)
        mass_part = jnp.sum(valid * mass)
        kcell = valid * counted
        cell_part = jnp.sum(kcell)
        spot_dot = jnp.sum(pred * target, axis=1)
        spot_pred = jnp.sum(pred * pred, axis=1)
        spot_true = jnp.sum(target * target, axis=1)
        gene_dot, gene_pred, gene_true, mass_total, cell_total = lax.psum(
            (gene_dot, gene_pred, gene_true, mass_part, cell_part), "spot"
        )
        spot_dot, spot_pred, spot_true = lax.psum((spot_dot, spot_pred, spot_true), "gene")
        gene_inv = lax.rsqrt(gene_pred * gene_true + tiny)
        cos_gene = gene_dot * gene_inv
        spot_inv = lax.rsqrt(spot_pred * spot_true + tiny)
        cos_spot = spot_dot * spot_inv
        share = kcell / cell_total
        scale_count = slide_spots[slide].astype(jnp.float32)
        kl_part = jnp.sum(
            share * (jnp.log(counted) - jnp.log(cell_total) - jnp.log(mass) + jnp.log(mass_total))
        )
        loss_local = loss_local - gene_share * jnp.sum(cos_gene)
        loss_local = loss_local + row_share * (scale_count * kl_part - jnp.sum(valid * cos_spot))
        gene_back = cos_gene * gene_true / (gene_pred * gene_true + tiny)
        spot_back = cos_spot * spot_true / (spot_pred * spot_true + tiny)
        dpred = -valid[:, None] * (
            target * (gene_inv[None, :] + spot_inv[:, None])
            - pred * gene_back[None, :]
            - pred * spot_back[:, None]
        )
        dmass = scale_count * valid * (1.0 / mass_total - share / mass)
        pred_list.append(pred)
        grads_full, mass_full = (
            lax.all_gather(dpred, "spot", axis=0, tiled=True),
            lax.all_gather(dmass, "spot", axis=0, tiled=True),
        )
        dprob_cells = jnp.dot(grads_full, expr.T, precision=lax.Precision.HIGHEST)
        dprob_cells = lax.psum(dprob_cells, "gene")
        expr_acc = expr_acc + lax.dot_general(
            blocks, grads_full, (((0,), (0,)), ((), ())), precision=lax.Precision.HIGHEST
        )
        dprob_cells = dprob_cells + mass_full[:, None] * own_weights[None, :]
        dprob_rows = lax.all_to_all(dprob_cells, "spot", split_axis=0, concat_axis=1, tiled=True)
        inner = jnp.sum(probs * dprob_rows, axis=1, keepdims=True)
        dlogit = probs * (dprob_rows - inner)
        grad_list.append(dlogit)
    loss = lax.psum(loss_local, ("spot", "gene"))
    return (jnp.stack(pred_list), loss, jnp.stack(grad_list), expr_acc)


def solution(mesh):
    places = mesh.shape["spot"]

    def on_device(logits, expr, spatial, slide_spots, spot_cells, cell_prior):
        if places == PLANE * PLANE and mesh.shape["gene"] == 2 and expr.shape[1] == sum(FORWARD):
            return plane_call(
                logits, expr, spatial, slide_spots, spot_cells, cell_prior, places // PLANE
            )
        return general_plan(logits, expr, spatial, slide_spots, spot_cells, cell_prior)

    in_specs = (
        P(None, "spot", None),
        P("spot", "gene"),
        P(None, "spot", "gene"),
        P(),
        P(None, "spot"),
        P(),
    )
    out_specs = (P(None, "spot", "gene"), P(), P(None, "spot", None), P("spot", "gene"))
    return jax.shard_map(
        on_device, mesh=mesh, in_specs=in_specs, out_specs=out_specs, check_vma=False
    )
```

```python
import functools

import jax
import jax.numpy as jnp
from jax import lax
from jax.experimental import pallas as pl
from jax.experimental.pallas import tpu as pltpu
from jax.sharding import PartitionSpec as P

tiny = 1e-06
fixed_point = 16384.0
F32 = jnp.float32
BF16 = jnp.bfloat16
MESH = pl.DeviceIdType.MESH

PLANE = 4
LANES = 128
STEP_ROWS = 16
FORWARD = (256, 128, 128, 128, 128, 128, 128)
BACKWARD = (128, 128, 128, 256, 256, 128)
SPLIT = 3
LEAD = 2
EARLY = 5
STEPS = (
    ("share",),
    ("far", 0),
    ("far", 1),
    ("near", 0),
    ("take",),
    ("turn", 0),
    ("whole", 0),
    ("near", 1),
    ("product", 0),
    ("far", 2),
    ("far", 3),
    ("whole", 1),
    ("far", 4),
    ("far", 5),
    ("product", 1),
    ("whole", 2),
    ("near", 2),
    ("near", 3),
    ("near", 4),
    ("product", 2),
    ("near", 5),
    ("sum", 0),
    ("whole", 3),
    ("product", 3),
    ("whole", 4),
    ("product", 4),
    ("sum", 1),
    ("whole", 5),
    ("sum", 2),
    ("far", 6),
    ("product", 5),
    ("sum", 3),
    ("near", 6),
    ("whole", 6),
    ("product", 6),
    ("sum", 4),
    ("plane", 0),
    ("sum", 5),
    ("sum", 6),
    ("plane", 1),
    ("cores",),
    ("line", 0),
    ("spots",),
    ("line", 1),
    ("genes", 0),
    ("grad", 0),
    ("grad", 1),
    ("turn", 1),
    ("grad", 2),
    ("genes", 1),
    ("backward", 0),
    ("grad", 3),
    ("backward", 1),
    ("grad", 4),
    ("probs", 0),
    ("probs", 1),
    ("add_near", 0),
    ("backward", 2),
    ("grad", 5),
    ("backward", 3),
    ("probs", 2),
    ("probs", 3),
    ("add_near", 1),
    ("backward", 4),
    ("add_far", 0),
    ("probs", 4),
    ("add_far", 1),
    ("add_near", 2),
    ("backward", 5),
    ("probs", 5),
    ("exchange",),
    ("add_near", 3),
    ("expr", 0),
    ("add_far", 2),
    ("return",),
    ("add_near", 4),
    ("add_far", 3),
    ("add_far", 4),
    ("terms",),
    ("expr", 1),
    ("loss",),
    ("logits",),
    ("expr", 2),
    ("expr", 3),
    ("add_near", 5),
    ("expr", 4),
    ("add_far", 5),
    ("expr", 5),
)


def halves(value):
    high = value.astype(BF16)
    return high, (value - high.astype(F32)).astype(BF16)


def product(a_high, a_low, b_high, b_low, contract):
    def one(a, b):
        return lax.dot_general(a, b, (contract, ((), ())), preferred_element_type=F32)

    return one(a_high, b_high) + (one(a_high, b_low) + one(a_low, b_high))


def plane_kernel(lines, forward_widths, backward_widths, *refs):
    chunks, turns = len(forward_widths), len(backward_widths)
    (
        (logits_ref, expr_ref, spatial_ref, count_in, cells_in, prior_in),
        (pr, loss_ref, glog, ge),
        (count_ref, cells_ref, prior_ref, lg, lq, tg, ex, pq, ab, af, ahi, alo, thi, tlo, bhi, blo, sacc, s1, s2, gv, ss, rowv, rs),
        (dhi, dlo, fs, fx, fy, fz, fr, inn, l1, l2),
        (loc, ou_s, ou_r, od_s, od_r, fu_s, fu_r, fd_s, fd_r, a_s, a_r, a2_s, a2_r, r_s, r_r),
        (c_s, c_r, s1_s, s1_r, s2_s, s2_r, ss_s, ss_r, d_s, d_r, ru_s, ru_r, rd_s, rd_r),
        (f_s, f_r, fx_s, fx_r, go_s, go_r, in_s, in_r, l1_s, l1_r, l2_s, l2_r),
        bb,
        cs,
        cr,
        ds,
        es,
        ru,
        rd,
    ) = grouped(refs, (6, 4, 23, 10, 15, 14, 12, chunks, chunks, chunks, turns, turns, turns, turns))
    place = lax.axis_index("spot")
    core = lax.axis_index("gene")
    z = place // PLANE
    q = place % PLANE
    col, row = q % 2, q // 2
    mates = ((1 - row) * 2 + 1 - col, row * 2 + 1 - col, (1 - row) * 2 + col)
    others = tuple((z + step) % lines for step in range(1, lines))
    up, down = (place + PLANE, core), (place - PLANE, core)
    sibling = (place, 1 - core)
    slides, slide_rows = logits_ref.shape[0], logits_ref.shape[1]
    rows = slides * slide_rows
    cb = expr_ref.shape[0]
    genes = expr_ref.shape[1]
    last = lines - 1

    def mate(p):
        return (z * PLANE + p, core)

    def send(src, dst, send_sem, recv_sem, device):
        copy = pltpu.make_async_remote_copy(
            src_ref=src, dst_ref=dst, send_sem=send_sem, recv_sem=recv_sem, device_id=device, device_id_type=MESH
        )
        copy.start()

    def arrived(dst, recv_sem):
        pltpu.make_async_copy(dst, dst, recv_sem).wait()

    sent = arrived

    def cols(k):
        return pl.ds(sum(forward_widths[:k]), forward_widths[k])

    def turn_cols(k):
        return pl.ds(sum(backward_widths[:k]), backward_widths[k])

    def block(index):
        return pl.ds(pl.multiple_of(index * cb, cb), cb)

    def share(index):
        return pl.ds(pl.multiple_of(index * rows, rows), rows)

    def half(index):
        return pl.ds(pl.multiple_of(index * slide_rows, slide_rows), slide_rows)

    small = ((prior_in, prior_ref), (count_in, count_ref), (cells_in, cells_ref))
    pltpu.make_async_copy(expr_ref, ex, loc.at[2 * slides]).start()
    for m in range(slides):
        pltpu.make_async_copy(logits_ref.at[m], lg.at[half(m)], loc.at[m]).start()
    for at, (src, dst) in enumerate(small):
        pltpu.make_async_copy(src, dst, loc.at[2 * slides + 1 + at]).start()
    for m in range(slides):
        pltpu.make_async_copy(spatial_ref.at[m], tg.at[half(m)], loc.at[slides + m]).start()

    barrier = pltpu.get_barrier_semaphore()
    for p in mates:
        pl.semaphore_signal(barrier, inc=1, device_id=mate(p), device_id_type=MESH)
    for o in others:
        pl.semaphore_signal(barrier, inc=1, device_id=(o * PLANE + q, core), device_id_type=MESH)
    pl.semaphore_signal(barrier, inc=1, device_id=sibling, device_id_type=MESH)
    pltpu.make_async_copy(expr_ref, ex, loc.at[2 * slides]).wait()
    for k in range(chunks):
        bb[k][block(z), :] = ex[:, cols(k)]
    for m in range(slides):
        pltpu.make_async_copy(logits_ref.at[m], lg.at[half(m)], loc.at[m]).wait()
    for p in range(PLANE):
        for line in range(lines):
            lq[p, :, pl.ds(line * cb, cb)] = lg[half(core), pl.ds((line * PLANE + p) * cb, cb)]
    pl.semaphore_wait(barrier, len(mates) + len(others) + 1)

    def own_up(k):
        here = bb[k].at[block(z)]
        send(here, here, ou_s.at[k], ou_r.at[k], up)

    def own_down(k):
        here = bb[k].at[block(z)]
        send(here, here, od_s.at[k], od_r.at[k], down)

    def low(at):
        return 2 * at < lines

    for at in range(lines):

        @pl.when(z == at)
        def _():
            for k in range(chunks):
                if at < last and (not low(at) or at == 0 or k < LEAD):
                    own_up(k)
                if at > 0 and (low(at) or at == last or k < LEAD):
                    own_down(k)

    for p in mates:
        send(lq.at[p], ab.at[q, half(core)], a_s, a_r.at[q], mate(p))

    def from_below(k, at):
        arrived(bb[k].at[pl.ds((at - 1) * cb, cb)], ou_r.at[k])
        if at > 1:
            arrived(bb[k].at[pl.ds(0, (at - 1) * cb)], fu_r.at[k])

    def from_above(k, at):
        arrived(bb[k].at[pl.ds((at + 1) * cb, cb)], od_r.at[k])
        if at < last - 1:
            arrived(bb[k].at[pl.ds((at + 2) * cb, (last - 1 - at) * cb)], fd_r.at[k])

    def upward(k, at):
        from_below(k, at)
        here = bb[k].at[pl.ds(0, at * cb)]
        send(here, here, fu_s.at[k], fu_r.at[k], up)

    def downward(k, at):
        from_above(k, at)
        here = bb[k].at[pl.ds((at + 1) * cb, (last - at) * cb)]
        send(here, here, fd_s.at[k], fd_r.at[k], down)

    def forward_far(k):
        for at in range(1, last):

            @pl.when(z == at)
            def _():
                (upward if low(at) else downward)(k, at)
                if k + LEAD < chunks:
                    (own_up if low(at) else own_down)(k + LEAD)

    def forward_near(k):
        for at in range(1, last):

            @pl.when(z == at)
            def _():
                (downward if low(at) else upward)(k, at)

    def gathered(k):
        @pl.when(z == 0)
        def _():
            from_above(k, 0)

        @pl.when(z == last)
        def _():
            from_below(k, last)

    for at, (src, dst) in enumerate(small):
        pltpu.make_async_copy(src, dst, loc.at[2 * slides + 1 + at]).wait()
    weights = prior_ref[...].astype(F32) / fixed_point

    @pl.loop(0, rows // STEP_ROWS)
    def _(step):
        at = pl.ds(pl.multiple_of(step * STEP_ROWS, STEP_ROWS), STEP_ROWS)
        value = lg[at, :]
        peak = jnp.max(value, axis=1, keepdims=True)
        raised = jnp.exp(value - peak)
        scale = 1.0 / jnp.sum(raised, axis=1, keepdims=True)
        probs = raised * scale
        mass_rows = jnp.sum(probs * weights, axis=1, keepdims=True)
        rowv[0, at, :] = jnp.broadcast_to(mass_rows, (STEP_ROWS, LANES))
        rowv[1, at, :] = jnp.broadcast_to(peak, (STEP_ROWS, LANES))
        rowv[2, at, :] = jnp.broadcast_to(scale, (STEP_ROWS, LANES))
        for p in range(PLANE):
            for line in range(lines):
                at_cells = (line * PLANE + p) * cb
                pq[p, at, pl.ds(line * cb, cb)] = probs[:, at_cells : at_cells + cb]

    wide = lax.broadcasted_iota(jnp.int32, (rows, LANES), 1)
    rs[q] = jnp.where(wide == 0, rowv[1], rowv[2]).T[0:8]
    for p in mates:
        send(rs.at[q], rs.at[q], r_s, r_r.at[q], mate(p))

    rid = lax.broadcasted_iota(jnp.int32, (rows, 1), 0)
    first = rid < slide_rows
    position = place * slide_rows + jnp.where(first, rid, rid - slide_rows)
    count = jnp.where(first, count_ref[0], count_ref[1])
    valid = (position < count).astype(F32)
    scale_count = count.astype(F32)
    square = (slide_rows, slide_rows)
    eye = lax.broadcasted_iota(jnp.int32, square, 0) == lax.broadcasted_iota(jnp.int32, square, 1)
    counted = jnp.concatenate(
        [
            jnp.sum(jnp.where(eye, cells_ref[m : m + 1, :].astype(F32), 0.0), axis=1, keepdims=True)
            for m in range(slides)
        ],
        axis=0,
    )
    mass = rowv[0, :, 0:1]
    kcell = valid * counted

    def by_slide(value):
        return [jnp.sum(value[m * slide_rows : (m + 1) * slide_rows], axis=0, keepdims=True) for m in range(slides)]

    mass_parts = by_slide(valid * mass)
    cell_parts = by_slide(kcell)
    lane = lax.broadcasted_iota(jnp.int32, (1, LANES), 1)
    scalars = jnp.zeros((1, LANES), F32)
    for at, value in enumerate(mass_parts + cell_parts):
        scalars = jnp.where(lane == at, value, scalars)
    for m in range(slides):
        pltpu.make_async_copy(spatial_ref.at[m], tg.at[half(m)], loc.at[slides + m]).wait()
    sacc[...] = jnp.zeros_like(sacc)
    s1[q, 3 * slides :, :] = jnp.zeros((8 - 3 * slides, genes), F32)
    s1[q, 3 * slides : 3 * slides + 1, 0:LANES] = scalars

    def share_logits():
        for p in (mates[1], mates[2], mates[0]):
            here = ab.at[p, half(core)]
            arrived(here, a_r.at[p])
            send(here, here, a2_s, a2_r.at[p], sibling)

    def take_probs():
        af[q] = pq[q]
        ahi[share(q), :], alo[share(q), :] = halves(pq[q])
        for p in (mates[1], mates[2], mates[0]):
            arrived(rs.at[p], r_r.at[p])
            arrived(ab.at[p, half(1 - core)], a2_r.at[p])
            by_row = rs[p].T
            probs = jnp.exp(ab[p] - by_row[:, 0:1]) * by_row[:, 1:2]
            af[p] = probs
            ahi[share(p), :], alo[share(p), :] = halves(probs)

    def transpose(part):
        for p in (2 * part, 2 * part + 1):
            high, low_part = halves(af[p].T)
            thi[:, share(p)], tlo[:, share(p)] = high, low_part

    def forward_product(k):
        high, low = halves(bb[k][...])
        bhi[:, cols(k)], blo[:, cols(k)] = high, low
        if k < chunks - 1:
            cs[k][...] = product(ahi[...], alo[...], high, low, ((1,), (0,)))
            for p in mates:
                pass_pred(k, p)
        else:
            for side, served in ((1 - row, (mates[0], mates[2])), (row, (mates[1],))):
                pair = pl.ds(pl.multiple_of(2 * side * rows, 2 * rows), 2 * rows)
                cs[k][pair, :] = product(ahi[pair, :], alo[pair, :], high, low, ((1,), (0,)))
                for p in served:
                    pass_pred(k, p)

    def pass_pred(k, p):
        send(cs[k].at[share(p)], cr[k].at[q], c_s.at[k], c_r.at[k, q], mate(p))

    def finish_pred(k):
        total = cs[k][share(q), :]
        for p in mates:
            arrived(cr[k].at[p], c_r.at[k, p])
            total = total + cr[k][p]
        pr[:, cols(k)] = total
        truth = tg[:, cols(k)]
        for at, value in enumerate((total * truth, total * total, truth * truth)):
            sacc[at] += lane_groups(value)
        kept = valid * total
        stats = by_slide(kept * truth) + by_slide(kept * total) + by_slide(valid * truth * truth)
        s1[q, 0 : 3 * slides, cols(k)] = jnp.concatenate(stats, axis=0)

    early = sum(forward_widths[:EARLY])
    parts = (pl.ds(0, early), pl.ds(early, genes - early))

    def sum_plane(at):
        for p in mates:
            send(s1.at[q, :, parts[at]], s1.at[q, :, parts[at]], s1_s, s1_r.at[at, q], mate(p))

    def sum_line(at):
        for p in mates:
            arrived(s1.at[p, :, parts[at]], s1_r.at[at, p])
        s2[z, :, parts[at]] = (s1[0, :, parts[at]] + s1[1, :, parts[at]]) + (s1[2, :, parts[at]] + s1[3, :, parts[at]])
        for o in others:
            send(s2.at[z, :, parts[at]], s2.at[z, :, parts[at]], s2_s, s2_r.at[at, z], (o * PLANE + q, core))

    kept = {}

    def finish_genes(at):
        for o in others:
            arrived(s2.at[o, :, parts[at]], s2_r.at[at, o])
        total = s2[0, :, parts[at]]
        for line in range(1, lines):
            total = total + s2[line, :, parts[at]]
        gene_dot, gene_pred, gene_true = total[0:2], total[2:4], total[4:6]
        gene_inv = lax.rsqrt(gene_pred * gene_true + tiny)
        cos_gene = gene_dot * gene_inv
        gv[0:2, parts[at]] = gene_inv
        gv[2:4, parts[at]] = cos_gene * gene_true / (gene_pred * gene_true + tiny)
        kept["genes", at] = jnp.sum(jnp.sum(cos_gene, axis=1, keepdims=True), axis=0, keepdims=True)
        if at == 0:
            kept["mass"] = jnp.where(first, total[6:7, 0:1], total[6:7, 1:2])
            kept["cells"] = jnp.where(first, total[6:7, 2:3], total[6:7, 3:4])

    def sum_cores():
        sums = [jnp.sum(sacc[at], axis=1, keepdims=True) for at in range(3)]
        ss[core] = jnp.where(wide == 0, sums[0], jnp.where(wide == 1, sums[1], sums[2]))
        send(ss.at[core], ss.at[core], ss_s, ss_r, sibling)

    def finish_spots():
        arrived(ss.at[1 - core], ss_r)
        spot = ss[0] + ss[1]
        spot_dot, spot_pred, spot_true = spot[:, 0:1], spot[:, 1:2], spot[:, 2:3]
        spot_inv = lax.rsqrt(spot_pred * spot_true + tiny)
        cos_spot = spot_dot * spot_inv
        kept["inverse"], kept["cos"] = spot_inv, cos_spot
        kept["back"] = cos_spot * spot_true / (spot_pred * spot_true + tiny)
        sacc[0] = jnp.zeros_like(sacc[0])

    def send_grad(k):
        spot_inv, spot_back = kept["inverse"], kept["back"]
        pieces = []
        for m in range(slides):
            lo, hi = m * slide_rows, (m + 1) * slide_rows
            truth, guess = tg[lo:hi, turn_cols(k)], pr[lo:hi, turn_cols(k)]
            inverse, back = gv[m : m + 1, turn_cols(k)], gv[2 + m : 3 + m, turn_cols(k)]
            pieces.append(
                -valid[lo:hi]
                * (truth * (inverse + spot_inv[lo:hi]) - guess * back - guess * spot_back[lo:hi])
            )
        grad = jnp.concatenate(pieces, axis=0)
        here = ds[k].at[share(q)]
        here[...] = grad
        for p in mates:
            send(here, here, d_s.at[k], d_r.at[k, q], mate(p))
        sacc[0] += lane_groups(grad * pr[:, turn_cols(k)])

    def send_terms():
        mass_total, cell_total = kept["mass"], kept["cells"]
        portion = kcell / cell_total
        kl_rows = portion * (jnp.log(counted) - jnp.log(cell_total) - jnp.log(mass) + jnp.log(mass_total))
        dmass = scale_count * valid * (1.0 / mass_total - portion / mass)
        terms = jnp.sum(scale_count * kl_rows - valid * kept["cos"], axis=0, keepdims=True)
        l1[q] = jnp.broadcast_to(terms, (8, LANES))
        for p in mates:
            send(l1.at[q], l1.at[q], l1_s, l1_r.at[q], mate(p))
        inner = jnp.sum(sacc[0], axis=1, keepdims=True)
        inn[core] = jnp.where(wide == 0, inner, kept["genes", 0] + kept["genes", 1])
        send(inn.at[core], inn.at[core], in_s, in_r, sibling)
        rowv[1] = jnp.broadcast_to(dmass, (rows, LANES))

    middle = lines // 2

    def backward_product(k):
        for p in mates:
            arrived(ds[k].at[share(p)], d_r.at[k, p])
        high, low_part = halves(ds[k][...])
        dhi[:, turn_cols(k)], dlo[:, turn_cols(k)] = high, low_part
        if not halved(k):
            es[k][...] = product(thi[...], tlo[...], high, low_part, ((1,), (0,)))

        for turn in range(2):
            if halved(k):
                side = (1 - z // middle) if turn == 0 else z // middle
                pair = pl.ds(pl.multiple_of(side * middle * cb, middle * cb), middle * cb)
                es[k][pair, :] = product(thi[pair, :], tlo[pair, :], high, low_part, ((1,), (0,)))

            @pl.when(z == 0)
            def _():
                if halved(k):
                    pass_up(k, middle if turn == 0 else 1, middle if turn == 0 else middle - 1, turn)
                elif whole(k):
                    if turn == 0:
                        pass_up(k, 1, last, 0)
                elif turn == 0:
                    for line in range(last, 0, -1):
                        pass_up(k, line, 1, line)

            @pl.when(z == last)
            def _():
                if halved(k):
                    pass_down(k, 0 if turn == 0 else middle, middle if turn == 0 else middle - 1, turn)
                elif whole(k):
                    if turn == 0:
                        pass_down(k, 0, last, 0)
                elif turn == 0:
                    for line in range(last):
                        pass_down(k, line, 1, line)

    def halved(k):
        return k == 0

    def whole(k):
        return 0 < k < turns - SPLIT

    def pass_up(k, line, count, slot):
        here = pl.ds(line * cb, count * cb)
        send(es[k].at[here], ru[k].at[here], ru_s.at[k], ru_r.at[k, slot], up)

    def pass_down(k, line, count, slot):
        here = pl.ds(line * cb, count * cb)
        send(es[k].at[here], rd[k].at[here], rd_s.at[k], rd_r.at[k, slot], down)

    def take_up(k, line, count, slot):
        arrived(ru[k].at[pl.ds(line * cb, count * cb)], ru_r.at[k, slot])

    def take_down(k, line, count, slot):
        arrived(rd[k].at[pl.ds(line * cb, count * cb)], rd_r.at[k, slot])

    def add_up(k, line, count):
        here = pl.ds(line * cb, count * cb)
        es[k][here, :] += ru[k][here, :]

    def add_down(k, line, count):
        here = pl.ds(line * cb, count * cb)
        es[k][here, :] += rd[k][here, :]

    def rising(k, at):
        if halved(k) or whole(k):
            start = middle if halved(k) else at
            take_up(k, start, lines - start, 0)
            above = max(at + 1, start)
            add_up(k, above, lines - above)
            pass_up(k, above, lines - above, 0)
        else:
            for line in range(last, at, -1):
                take_up(k, line, 1, line)
                add_up(k, line, 1)
                pass_up(k, line, 1, line)

    def falling(k, at):
        if halved(k) or whole(k):
            end = middle if halved(k) else at + 1
            take_down(k, 0, end, 0)
            below = min(at, end)
            add_down(k, 0, below)
            pass_down(k, 0, below, 0)
        else:
            for line in range(at):
                take_down(k, line, 1, line)
                add_down(k, line, 1)
                pass_down(k, line, 1, line)

    def add_near(k):
        for at in range(1, last):

            @pl.when(z == at)
            def _():
                (rising if low(at) else falling)(k, at)

    def add_far(k):
        for at in range(1, last):

            @pl.when(z == at)
            def _():
                (falling if low(at) else rising)(k, at)

    def finish_expr(k):
        for at in range(lines):

            @pl.when(z == at)
            def _():
                own = pl.ds(at * cb, cb)
                total = es[k][own, :]
                if at > 0:
                    if halved(k) and at < middle:
                        take_up(k, at, 1, 1)
                    elif at == last and (halved(k) or whole(k)):
                        take_up(k, at, 1, 0)
                    elif not halved(k) and not whole(k):
                        take_up(k, at, 1, at)
                    total = total + ru[k][own, :]
                if at < last:
                    if halved(k) and at >= middle:
                        take_down(k, at, 1, 1)
                    elif at == 0 and (halved(k) or whole(k)):
                        take_down(k, at, 1, 0)
                    elif not halved(k) and not whole(k):
                        take_down(k, at, 1, at)
                    total = total + rd[k][own, :]
                ge[:, turn_cols(k)] = total

    def probs_gradient(k):
        at = turn_cols(k)
        part = product(dhi[:, at], dlo[:, at], bhi[:, at], blo[:, at], ((1,), (1,)))
        if k == 0:
            fs[...] = part
        else:
            fs[...] += part

    def slide_of(p, m):
        return pl.ds(pl.multiple_of(p * rows + m * slide_rows, slide_rows), slide_rows)

    def sum_probs_cores():
        for p in mates + (q,):
            fx[p] = fs[slide_of(p, 1 - core), :]
            send(fx.at[p], fy.at[p], fx_s, fx_r.at[p], sibling)

    def return_probs():
        for p in mates + (q,):
            arrived(fy.at[p], fx_r.at[p])
            fz[p] = fs[slide_of(p, core), :] + fy[p]
        for p in mates:
            send(fz.at[p], fr.at[q], f_s, f_r.at[q], mate(p))
        fr[q] = fz[q]

    def pass_terms():
        for p in mates:
            arrived(l1.at[p], l1_r.at[p])
        l2[z] = (l1[0] + l1[1]) + (l1[2] + l1[3])
        for o in others:
            send(l2.at[z], l2.at[z], l2_s, l2_r.at[z], (o * PLANE + q, core))

    def part_of(slide, m):
        start = slide * slide_rows + m * (slide_rows // 2)
        return pl.ds(pl.multiple_of(start, slide_rows // 2), slide_rows // 2)

    def finish_logits():
        arrived(inn.at[1 - core], in_r)
        rowv[2] = (inn[0] + inn[1]) + rowv[1] * rowv[0]
        for p in mates:
            arrived(fr.at[p], f_r.at[p])
        for m in range(2):

            @pl.loop(0, slide_rows // STEP_ROWS // 2)
            def _(step):
                row_at = (m * (slide_rows // STEP_ROWS // 2) + step) * STEP_ROWS
                at = pl.ds(pl.multiple_of(row_at, STEP_ROWS), STEP_ROWS)
                whole_at = pl.ds(pl.multiple_of(core * slide_rows + row_at, STEP_ROWS), STEP_ROWS)
                by_mass, total_inner = rowv[1, whole_at, 0:1], rowv[2, whole_at, 0:1]
                for p in range(PLANE):
                    for line in range(lines):
                        here, there = pl.ds(line * cb, cb), (line * PLANE + p) * cb
                        grad = fr[p, at, here] + by_mass * weights[:, there : there + cb]
                        glog[whole_at, pl.ds(there, cb)] = pq[p, whole_at, here] * (grad - total_inner)

            here = part_of(core, m)
            send(glog.at[here], glog.at[here], go_s, go_r.at[m], sibling)

    steps = {
        "far": forward_far,
        "near": forward_near,
        "share": share_logits,
        "take": take_probs,
        "whole": gathered,
        "product": forward_product,
        "sum": finish_pred,
        "turn": transpose,
        "plane": sum_plane,
        "line": sum_line,
        "genes": finish_genes,
        "cores": sum_cores,
        "spots": finish_spots,
        "grad": send_grad,
        "terms": send_terms,
        "backward": backward_product,
        "probs": probs_gradient,
        "exchange": sum_probs_cores,
        "return": return_probs,
        "loss": pass_terms,
        "logits": finish_logits,
        "add_near": add_near,
        "add_far": add_far,
        "expr": finish_expr,
    }
    for name, *where in STEPS:
        steps[name](*where)

    for o in others:
        arrived(l2.at[o], l2_r.at[o])
    loss = l2[0]
    for line in range(1, lines):
        loss = loss + l2[line]
    loss_ref[...] = loss[0:1, 0:1] - (inn[0, 0:1, 1:2] + inn[1, 0:1, 1:2])
    for m in range(2):
        arrived(glog.at[part_of(1 - core, m)], go_r.at[m])

    for k in range(chunks):

        @pl.when(z < last)
        def _():
            sent(bb[k].at[block(z)], ou_s.at[k])

        @pl.when(z > 0)
        def _():
            sent(bb[k].at[block(z)], od_s.at[k])

        for at in range(1, last):

            @pl.when(z == at)
            def _():
                sent(bb[k].at[pl.ds(0, at * cb)], fu_s.at[k])
                sent(bb[k].at[pl.ds((at + 1) * cb, (last - at) * cb)], fd_s.at[k])

    for k in range(turns):
        for at in range(lines):

            @pl.when(z == at)
            def _():
                if at < last:
                    sent(es[k].at[pl.ds((at + 1) * cb, (last - at) * cb)], ru_s.at[k])
                if at > 0:
                    sent(es[k].at[pl.ds(0, at * cb)], rd_s.at[k])

    three = pl.ds(0, len(mates))
    sent(ab.at[three, half(0)], a_s)
    sent(ab.at[three, half(0)], a2_s)
    sent(rs.at[three], r_s)
    for k in range(chunks):
        sent(cr[k].at[three], c_s.at[k])
    sent(s1.at[three], s1_s)
    sent(s2.at[pl.ds(0, last)], s2_s)
    sent(ss.at[0], ss_s)
    for k in range(turns):
        sent(ds[k].at[pl.ds(0, len(mates) * rows)], d_s.at[k])
    sent(inn.at[0], in_s)
    sent(l1.at[three], l1_s)
    sent(l2.at[pl.ds(0, last)], l2_s)
    sent(fr.at[three], f_s)
    sent(fx, fx_s)
    sent(glog.at[half(0)], go_s)


def lane_groups(value):
    parts = [value[:, at : at + LANES] for at in range(0, value.shape[1], LANES)]
    return functools.reduce(lambda a, b: a + b, parts)


def grouped(refs, sizes):
    at = 0
    for size in sizes:
        yield refs[at : at + size]
        at += size


def deliver(pred_in, loss_in, glog_in, gexp_in, pred_ref, loss_ref, glog_ref, gexp_ref, sems):
    slides, slide_rows = pred_ref.shape[0], pred_ref.shape[1]
    copies = []
    quarter = slide_rows // 4
    for at in range(4 * slides):
        part, where = pl.ds(at * quarter, quarter), pl.ds(at % 4 * quarter, quarter)
        copies.append(pltpu.make_async_copy(glog_in.at[part], glog_ref.at[at // 4, where], sems.at[0, at]))
        copies.append(pltpu.make_async_copy(pred_in.at[part], pred_ref.at[at // 4, where], sems.at[1, at]))
        copies.append(pltpu.make_async_copy(gexp_in.at[part], gexp_ref.at[part], sems.at[2, at]))
    for copy in copies:
        copy.start()
    loss_ref[...] = loss_in[...]
    for copy in copies:
        copy.wait()


def plane_call(logits, expr, spatial, slide_spots, spot_cells, cell_prior, lines):
    slides, slide_rows, cells = logits.shape
    rows = slides * slide_rows
    cb, genes = expr.shape
    quarter = lines * cb
    spots = PLANE * rows
    chunks, turns = len(FORWARD), len(BACKWARD)
    dma = pltpu.SemaphoreType.DMA
    vmem = pltpu.VMEM
    anywhere = pl.BlockSpec(memory_space=pl.ANY)
    in_vmem = pl.BlockSpec(memory_space=pltpu.VMEM)
    scratch = [
        pltpu.SMEM((slides,), jnp.int32),
        vmem((slides, slide_rows), jnp.int32),
        vmem((1, cells), jnp.int32),
        vmem((rows, cells), F32),
        vmem((PLANE, slide_rows, quarter), F32),
        vmem((rows, genes), F32),
        vmem((cb, genes), F32),
        vmem((PLANE, rows, quarter), F32),
        vmem((PLANE, rows, quarter), F32),
        vmem((PLANE, rows, quarter), F32),
        vmem((spots, quarter), BF16),
        vmem((spots, quarter), BF16),
        vmem((quarter, spots), BF16),
        vmem((quarter, spots), BF16),
        vmem((quarter, genes), BF16),
        vmem((quarter, genes), BF16),
        vmem((3, rows, LANES), F32),
        vmem((PLANE, 8, genes), F32),
        vmem((lines, 8, genes), F32),
        vmem((8, genes), F32),
        vmem((2, rows, LANES), F32),
        vmem((3, rows, LANES), F32),
        vmem((PLANE, 8, rows), F32),
        vmem((spots, genes), BF16),
        vmem((spots, genes), BF16),
        vmem((spots, quarter), F32),
        vmem((PLANE, slide_rows, quarter), F32),
        vmem((PLANE, slide_rows, quarter), F32),
        vmem((PLANE, slide_rows, quarter), F32),
        vmem((PLANE, slide_rows, quarter), F32),
        vmem((2, rows, LANES), F32),
        vmem((PLANE, 8, LANES), F32),
        vmem((lines, 8, LANES), F32),
        dma((2 * slides + 4,)),
        dma((chunks,)),
        dma((chunks,)),
        dma((chunks,)),
        dma((chunks,)),
        dma((chunks,)),
        dma((chunks,)),
        dma((chunks,)),
        dma((chunks,)),
        dma,
        dma((PLANE,)),
        dma,
        dma((PLANE,)),
        dma,
        dma((PLANE,)),
        dma((chunks,)),
        dma((chunks, PLANE)),
        dma,
        dma((2, PLANE)),
        dma,
        dma((2, lines)),
        dma,
        dma,
        dma((turns,)),
        dma((turns, PLANE)),
        dma((turns,)),
        dma((turns, lines)),
        dma((turns,)),
        dma((turns, lines)),
        dma,
        dma((PLANE,)),
        dma,
        dma((PLANE,)),
        dma,
        dma((2,)),
        dma,
        dma,
        dma,
        dma((PLANE,)),
        dma,
        dma((lines,)),
    ]
    for shape, widths in (
        ((quarter,), FORWARD),
        ((spots,), FORWARD),
        ((PLANE, rows), FORWARD),
        ((spots,), BACKWARD),
        ((quarter,), BACKWARD),
        ((quarter,), BACKWARD),
        ((quarter,), BACKWARD),
    ):
        scratch += [vmem(shape + (width,), F32) for width in widths]
    in_hbm = functools.partial(pltpu.with_memory_space_constraint, memory_space=pltpu.HBM)
    in_place = functools.partial(pltpu.with_memory_space_constraint, memory_space=pltpu.VMEM)
    results = pl.pallas_call(
        functools.partial(plane_kernel, lines, FORWARD, BACKWARD),
        out_shape=(
            vmem((rows, genes), F32),
            jax.ShapeDtypeStruct((1, 1), F32),
            vmem((rows, cells), F32),
            vmem((cb, genes), F32),
        ),
        in_specs=[anywhere] * 6,
        out_specs=(in_vmem,) * 4,
        scratch_shapes=scratch,
        compiler_params=pltpu.CompilerParams(
            collective_id=0, has_side_effects=True, vmem_limit_bytes=48 * 1024 * 1024
        ),
    )(*map(in_hbm, (logits, expr, spatial, slide_spots, spot_cells, cell_prior.reshape(1, cells))))
    pred, loss, grad_logits, grad_expr = pl.pallas_call(
        deliver,
        out_shape=(
            jax.ShapeDtypeStruct((slides, slide_rows, genes), F32),
            jax.ShapeDtypeStruct((1, 1), F32),
            jax.ShapeDtypeStruct((slides, slide_rows, cells), F32),
            jax.ShapeDtypeStruct((cb, genes), F32),
        ),
        in_specs=[anywhere, in_vmem, anywhere, anywhere],
        out_specs=(anywhere, in_vmem, anywhere, anywhere),
        scratch_shapes=[dma((3, 4 * slides))],
        compiler_params=pltpu.CompilerParams(vmem_limit_bytes=4 * 1024 * 1024),
    )(in_place(results[0]), results[1], in_place(results[2]), in_place(results[3]))
    return pred, loss.reshape(()), grad_logits, grad_expr


def general_plan(logits, expr, spatial, slide_spots, spot_cells, cell_prior):
    place = lax.axis_index("spot")
    side = lax.axis_index("gene")
    rows_all = logits.shape[1]
    cell_rows = expr.shape[0]
    weights = cell_prior.astype(jnp.float32) / fixed_point
    gene_share = (place == 0).astype(jnp.float32)
    row_share = (side == 0).astype(jnp.float32)
    own_weights = lax.dynamic_slice_in_dim(weights, place * cell_rows, cell_rows, 0)
    expr_acc = jnp.zeros((cell_rows, expr.shape[1]), jnp.float32)
    loss_local = jnp.zeros((), jnp.float32)
    pred_list = []
    grad_list = []
    for slide in range(logits.shape[0]):
        logit_rows = logits[slide]
        counted = spot_cells[slide].astype(jnp.float32)
        target = spatial[slide]
        positions = place * rows_all + jnp.arange(rows_all, dtype=jnp.int32)
        valid = (positions < slide_spots[slide]).astype(jnp.float32)
        peak = jnp.max(logit_rows, axis=1, keepdims=True)
        raised = jnp.exp(logit_rows - peak)
        probs = raised / jnp.sum(raised, axis=1, keepdims=True)
        mass = jnp.dot(probs, weights, precision=lax.Precision.HIGHEST)
        blocks = lax.all_to_all(probs, "spot", split_axis=1, concat_axis=0, tiled=True)
        pred = lax.psum_scatter(
            jnp.dot(blocks, expr, precision=lax.Precision.HIGHEST),
            "spot",
            scatter_dimension=0,
            tiled=True,
        )
        gene_dot = jnp.sum(valid[:, None] * pred * target, axis=0)
        gene_pred = jnp.sum(valid[:, None] * pred * pred, axis=0)
        gene_true = jnp.sum(valid[:, None] * target * target, axis=0)
        mass_part = jnp.sum(valid * mass)
        kcell = valid * counted
        cell_part = jnp.sum(kcell)
        spot_dot = jnp.sum(pred * target, axis=1)
        spot_pred = jnp.sum(pred * pred, axis=1)
        spot_true = jnp.sum(target * target, axis=1)
        gene_dot, gene_pred, gene_true, mass_total, cell_total = lax.psum(
            (gene_dot, gene_pred, gene_true, mass_part, cell_part), "spot"
        )
        spot_dot, spot_pred, spot_true = lax.psum((spot_dot, spot_pred, spot_true), "gene")
        gene_inv = lax.rsqrt(gene_pred * gene_true + tiny)
        cos_gene = gene_dot * gene_inv
        spot_inv = lax.rsqrt(spot_pred * spot_true + tiny)
        cos_spot = spot_dot * spot_inv
        share = kcell / cell_total
        scale_count = slide_spots[slide].astype(jnp.float32)
        kl_part = jnp.sum(
            share * (jnp.log(counted) - jnp.log(cell_total) - jnp.log(mass) + jnp.log(mass_total))
        )
        loss_local = loss_local - gene_share * jnp.sum(cos_gene)
        loss_local = loss_local + row_share * (scale_count * kl_part - jnp.sum(valid * cos_spot))
        gene_back = cos_gene * gene_true / (gene_pred * gene_true + tiny)
        spot_back = cos_spot * spot_true / (spot_pred * spot_true + tiny)
        dpred = -valid[:, None] * (
            target * (gene_inv[None, :] + spot_inv[:, None])
            - pred * gene_back[None, :]
            - pred * spot_back[:, None]
        )
        dmass = scale_count * valid * (1.0 / mass_total - share / mass)
        pred_list.append(pred)
        grads_full, mass_full = (
            lax.all_gather(dpred, "spot", axis=0, tiled=True),
            lax.all_gather(dmass, "spot", axis=0, tiled=True),
        )
        dprob_cells = jnp.dot(grads_full, expr.T, precision=lax.Precision.HIGHEST)
        dprob_cells = lax.psum(dprob_cells, "gene")
        expr_acc = expr_acc + lax.dot_general(
            blocks, grads_full, (((0,), (0,)), ((), ())), precision=lax.Precision.HIGHEST
        )
        dprob_cells = dprob_cells + mass_full[:, None] * own_weights[None, :]
        dprob_rows = lax.all_to_all(dprob_cells, "spot", split_axis=0, concat_axis=1, tiled=True)
        inner = jnp.sum(probs * dprob_rows, axis=1, keepdims=True)
        dlogit = probs * (dprob_rows - inner)
        grad_list.append(dlogit)
    loss = lax.psum(loss_local, ("spot", "gene"))
    return (jnp.stack(pred_list), loss, jnp.stack(grad_list), expr_acc)


def solution(mesh):
    places = mesh.shape["spot"]

    def on_device(logits, expr, spatial, slide_spots, spot_cells, cell_prior):
        if places == PLANE * PLANE and mesh.shape["gene"] == 2 and expr.shape[1] == sum(FORWARD):
            return plane_call(
                logits, expr, spatial, slide_spots, spot_cells, cell_prior, places // PLANE
            )
        return general_plan(logits, expr, spatial, slide_spots, spot_cells, cell_prior)

    in_specs = (
        P(None, "spot", None),
        P("spot", "gene"),
        P(None, "spot", "gene"),
        P(),
        P(None, "spot"),
        P(),
    )
    out_specs = (P(None, "spot", "gene"), P(), P(None, "spot", None), P("spot", "gene"))
    return jax.shard_map(
        on_device, mesh=mesh, in_specs=in_specs, out_specs=out_specs, check_vma=False
    )
```

```python
import functools

import jax
import jax.numpy as jnp
from jax import lax
from jax.experimental import pallas as pl
from jax.experimental.pallas import tpu as pltpu
from jax.sharding import PartitionSpec as P

tiny = 1e-06
fixed_point = 16384.0
F32 = jnp.float32
BF16 = jnp.bfloat16
MESH = pl.DeviceIdType.MESH

PLANE = 4
LANES = 128
STEP_ROWS = 16
FORWARD = (256, 256, 256, 256)
BACKWARD = (128, 128, 256, 256, 256)
SPLIT = 2
LEAD = 2
EARLY = 3
STEPS = (
    ("far", 0),
    ("far", 1),
    ("share",),
    ("near", 0),
    ("take",),
    ("whole", 0),
    ("product", 0),
    ("whole", 1),
    ("near", 1),
    ("product", 1),
    ("far", 2),
    ("far", 3),
    ("sum", 0),
    ("near", 2),
    ("whole", 2),
    ("product", 2),
    ("sum", 1),
    ("near", 3),
    ("whole", 3),
    ("product", 3),
    ("sum", 2),
    ("plane", 0),
    ("sum", 3),
    ("plane", 1),
    ("cores",),
    ("line", 0),
    ("spots",),
    ("genes", 0),
    ("grad", 0),
    ("grad", 1),
    ("turn", 0),
    ("grad", 2),
    ("line", 1),
    ("grad", 3),
    ("turn", 1),
    ("genes", 1),
    ("backward", 0),
    ("backward", 1),
    ("probs", 0),
    ("grad", 4),
    ("probs", 1),
    ("backward", 2),
    ("probs", 2),
    ("terms",),
    ("add_near", 0),
    ("backward", 3),
    ("add_near", 1),
    ("add_far", 0),
    ("probs", 3),
    ("add_near", 2),
    ("backward", 4),
    ("probs", 4),
    ("exchange",),
    ("add_far", 1),
    ("add_near", 3),
    ("return",),
    ("loss",),
    ("add_far", 2),
    ("expr", 0),
    ("expr", 1),
    ("add_far", 3),
    ("add_near", 4),
    ("expr", 2),
    ("expr", 3),
    ("add_far", 4),
    ("logits",),
    ("expr", 4),
)


def halves(value):
    high = value.astype(BF16)
    return high, (value - high.astype(F32)).astype(BF16)


def threefold(value, axis, mixed):
    high, low = halves(value)
    return jnp.concatenate([high, low, high] if mixed else [high, high, low], axis=axis)


def product(a, b, contract):
    return lax.dot_general(a, b, (contract, ((), ())), preferred_element_type=F32)


def plane_kernel(lines, forward_widths, backward_widths, *refs):
    chunks, turns = len(forward_widths), len(backward_widths)
    (
        (logits_ref, expr_ref, spatial_ref, count_in, cells_in, prior_in),
        (pr, loss_ref, glog, ge),
        (count_ref, cells_ref, prior_ref, lg, lq, tg, ex, pq, ab, af, probs_3, turned_3, expr_3, sacc, s1, s2, gv, ss, rowv, rs),
        (grad_3, fs, fx, fy, fz, fr, inn, l1, l2),
        (loc, ou_s, ou_r, od_s, od_r, fu_s, fu_r, fd_s, fd_r, a_s, a_r, a2_s, a2_r, r_s, r_r),
        (c_s, c_r, s1_s, s1_r, s2_s, s2_r, ss_s, ss_r, d_s, d_r, ru_s, ru_r, rd_s, rd_r),
        (f_s, f_r, fx_s, fx_r, go_s, go_r, in_s, in_r, l1_s, l1_r, l2_s, l2_r),
        bb,
        cs,
        cr,
        ds,
        es,
        ru,
        rd,
    ) = grouped(refs, (6, 4, 20, 9, 15, 14, 12, chunks, chunks, chunks, turns, turns, turns, turns))
    place = lax.axis_index("spot")
    core = lax.axis_index("gene")
    z = place // PLANE
    q = place % PLANE
    col, row = q % 2, q // 2
    mates = ((1 - row) * 2 + 1 - col, row * 2 + 1 - col, (1 - row) * 2 + col)
    others = tuple((z + step) % lines for step in range(1, lines))
    up, down = (place + PLANE, core), (place - PLANE, core)
    sibling = (place, 1 - core)
    slides, slide_rows = logits_ref.shape[0], logits_ref.shape[1]
    rows = slides * slide_rows
    cb = expr_ref.shape[0]
    genes = expr_ref.shape[1]
    last = lines - 1

    def mate(p):
        return (z * PLANE + p, core)

    def send(src, dst, send_sem, recv_sem, device):
        copy = pltpu.make_async_remote_copy(
            src_ref=src, dst_ref=dst, send_sem=send_sem, recv_sem=recv_sem, device_id=device, device_id_type=MESH
        )
        copy.start()

    def arrived(dst, recv_sem):
        pltpu.make_async_copy(dst, dst, recv_sem).wait()

    sent = arrived

    def cols(k):
        return pl.ds(sum(forward_widths[:k]), forward_widths[k])

    def turn_cols(k):
        return pl.ds(sum(backward_widths[:k]), backward_widths[k])

    def block(index):
        return pl.ds(pl.multiple_of(index * cb, cb), cb)

    def share(index):
        return pl.ds(pl.multiple_of(index * rows, rows), rows)

    def half(index):
        return pl.ds(pl.multiple_of(index * slide_rows, slide_rows), slide_rows)

    small = ((prior_in, prior_ref), (count_in, count_ref), (cells_in, cells_ref))
    pltpu.make_async_copy(expr_ref, ex, loc.at[2 * slides]).start()
    for m in range(slides):
        pltpu.make_async_copy(logits_ref.at[m], lg.at[half(m)], loc.at[m]).start()
    for at, (src, dst) in enumerate(small):
        pltpu.make_async_copy(src, dst, loc.at[2 * slides + 1 + at]).start()
    for m in range(slides):
        pltpu.make_async_copy(spatial_ref.at[m], tg.at[half(m)], loc.at[slides + m]).start()

    barrier = pltpu.get_barrier_semaphore()
    for p in mates:
        pl.semaphore_signal(barrier, inc=1, device_id=mate(p), device_id_type=MESH)
    for o in others:
        pl.semaphore_signal(barrier, inc=1, device_id=(o * PLANE + q, core), device_id_type=MESH)
    pl.semaphore_signal(barrier, inc=1, device_id=sibling, device_id_type=MESH)
    pltpu.make_async_copy(expr_ref, ex, loc.at[2 * slides]).wait()
    for k in range(chunks):
        bb[k][block(z), :] = ex[:, cols(k)]
    for m in range(slides):
        pltpu.make_async_copy(logits_ref.at[m], lg.at[half(m)], loc.at[m]).wait()
    for p in range(PLANE):
        for line in range(lines):
            lq[p, :, pl.ds(line * cb, cb)] = lg[half(core), pl.ds((line * PLANE + p) * cb, cb)]
    pl.semaphore_wait(barrier, len(mates) + len(others) + 1)

    def own_up(k):
        here = bb[k].at[block(z)]
        send(here, here, ou_s.at[k], ou_r.at[k], up)

    def own_down(k):
        here = bb[k].at[block(z)]
        send(here, here, od_s.at[k], od_r.at[k], down)

    def low(at):
        return 2 * at < lines

    for at in range(lines):

        @pl.when(z == at)
        def _():
            for k in range(chunks):
                if at < last and (not low(at) or at == 0 or k < LEAD):
                    own_up(k)
                if at > 0 and (low(at) or at == last or k < LEAD):
                    own_down(k)

    for p in mates:
        send(lq.at[p], ab.at[q, half(core)], a_s, a_r.at[q], mate(p))

    def from_below(k, at):
        arrived(bb[k].at[pl.ds((at - 1) * cb, cb)], ou_r.at[k])
        if at > 1:
            arrived(bb[k].at[pl.ds(0, (at - 1) * cb)], fu_r.at[k])

    def from_above(k, at):
        arrived(bb[k].at[pl.ds((at + 1) * cb, cb)], od_r.at[k])
        if at < last - 1:
            arrived(bb[k].at[pl.ds((at + 2) * cb, (last - 1 - at) * cb)], fd_r.at[k])

    def upward(k, at):
        from_below(k, at)
        here = bb[k].at[pl.ds(0, at * cb)]
        send(here, here, fu_s.at[k], fu_r.at[k], up)

    def downward(k, at):
        from_above(k, at)
        here = bb[k].at[pl.ds((at + 1) * cb, (last - at) * cb)]
        send(here, here, fd_s.at[k], fd_r.at[k], down)

    def forward_far(k):
        for at in range(1, last):

            @pl.when(z == at)
            def _():
                (upward if low(at) else downward)(k, at)
                if k + LEAD < chunks:
                    (own_up if low(at) else own_down)(k + LEAD)

    def forward_near(k):
        for at in range(1, last):

            @pl.when(z == at)
            def _():
                (downward if low(at) else upward)(k, at)

    def gathered(k):
        @pl.when(z == 0)
        def _():
            from_above(k, 0)

        @pl.when(z == last)
        def _():
            from_below(k, last)

    for at, (src, dst) in enumerate(small):
        pltpu.make_async_copy(src, dst, loc.at[2 * slides + 1 + at]).wait()
    weights = prior_ref[...].astype(F32) / fixed_point

    @pl.loop(0, rows // STEP_ROWS)
    def _(step):
        at = pl.ds(pl.multiple_of(step * STEP_ROWS, STEP_ROWS), STEP_ROWS)
        value = lg[at, :]
        peak = jnp.max(value, axis=1, keepdims=True)
        raised = jnp.exp(value - peak)
        scale = 1.0 / jnp.sum(raised, axis=1, keepdims=True)
        probs = raised * scale
        mass_rows = jnp.sum(probs * weights, axis=1, keepdims=True)
        rowv[0, at, :] = jnp.broadcast_to(mass_rows, (STEP_ROWS, LANES))
        rowv[1, at, :] = jnp.broadcast_to(peak, (STEP_ROWS, LANES))
        rowv[2, at, :] = jnp.broadcast_to(scale, (STEP_ROWS, LANES))
        for p in range(PLANE):
            for line in range(lines):
                at_cells = (line * PLANE + p) * cb
                pq[p, at, pl.ds(line * cb, cb)] = probs[:, at_cells : at_cells + cb]

    wide = lax.broadcasted_iota(jnp.int32, (rows, LANES), 1)
    rs[q] = jnp.where(wide == 0, rowv[1], rowv[2]).T[0:8]
    for p in mates:
        send(rs.at[q], rs.at[q], r_s, r_r.at[q], mate(p))

    rid = lax.broadcasted_iota(jnp.int32, (rows, 1), 0)
    first = rid < slide_rows
    position = place * slide_rows + jnp.where(first, rid, rid - slide_rows)
    count = jnp.where(first, count_ref[0], count_ref[1])
    valid = (position < count).astype(F32)
    scale_count = count.astype(F32)
    square = (slide_rows, slide_rows)
    eye = lax.broadcasted_iota(jnp.int32, square, 0) == lax.broadcasted_iota(jnp.int32, square, 1)
    counted = jnp.concatenate(
        [
            jnp.sum(jnp.where(eye, cells_ref[m : m + 1, :].astype(F32), 0.0), axis=1, keepdims=True)
            for m in range(slides)
        ],
        axis=0,
    )
    mass = rowv[0, :, 0:1]
    kcell = valid * counted

    def by_slide(value):
        return [jnp.sum(value[m * slide_rows : (m + 1) * slide_rows], axis=0, keepdims=True) for m in range(slides)]

    mass_parts = by_slide(valid * mass)
    cell_parts = by_slide(kcell)
    lane = lax.broadcasted_iota(jnp.int32, (1, LANES), 1)
    scalars = jnp.zeros((1, LANES), F32)
    for at, value in enumerate(mass_parts + cell_parts):
        scalars = jnp.where(lane == at, value, scalars)
    for m in range(slides):
        pltpu.make_async_copy(spatial_ref.at[m], tg.at[half(m)], loc.at[slides + m]).wait()
    sacc[...] = jnp.zeros_like(sacc)
    s1[q, 3 * slides :, :] = jnp.zeros((8 - 3 * slides, genes), F32)
    s1[q, 3 * slides : 3 * slides + 1, 0:LANES] = scalars

    def share_logits():
        for p in (mates[1], mates[2], mates[0]):
            here = ab.at[p, half(core)]
            arrived(here, a_r.at[p])
            send(here, here, a2_s, a2_r.at[p], sibling)

    def take_probs():
        af[q] = pq[q]
        probs_3[share(q), :] = threefold(pq[q], 1, False)
        for p in (mates[1], mates[2], mates[0]):
            arrived(rs.at[p], r_r.at[p])
            arrived(ab.at[p, half(1 - core)], a2_r.at[p])
            by_row = rs[p].T
            probs = jnp.exp(ab[p] - by_row[:, 0:1]) * by_row[:, 1:2]
            af[p] = probs
            probs_3[share(p), :] = threefold(probs, 1, False)

    def transpose(part):
        for p in (2 * part, 2 * part + 1):
            high, low_part = halves(af[p].T)
            for at, value in enumerate((high, high, low_part)):
                turned_3[:, pl.ds(at * PLANE * rows + p * rows, rows)] = value

    def keep_expr(k, value):
        start = sum(forward_widths[:k])
        for turn in range(turns):
            origin, width = sum(backward_widths[:turn]), backward_widths[turn]
            lo, hi = max(start, origin), min(start + forward_widths[k], origin + width)
            if lo < hi:
                high, low_part = halves(value[:, lo - start : hi - start])
                for at, part in enumerate((high, low_part, high)):
                    expr_3[:, pl.ds(3 * origin + at * width + lo - origin, hi - lo)] = part

    def three_turn_cols(k):
        return pl.ds(3 * sum(backward_widths[:k]), 3 * backward_widths[k])

    def forward_product(k):
        value = bb[k][...]
        factor = threefold(value, 0, True)
        keep_expr(k, value)
        if k < chunks - 1:
            cs[k][...] = product(probs_3[...], factor, ((1,), (0,)))
            for p in mates:
                pass_pred(k, p)
        else:
            for side, served in ((1 - row, (mates[0], mates[2])), (row, (mates[1],))):
                pair = pl.ds(pl.multiple_of(2 * side * rows, 2 * rows), 2 * rows)
                cs[k][pair, :] = product(probs_3[pair, :], factor, ((1,), (0,)))
                for p in served:
                    pass_pred(k, p)

    def pass_pred(k, p):
        send(cs[k].at[share(p)], cr[k].at[q], c_s.at[k], c_r.at[k, q], mate(p))

    def finish_pred(k):
        total = cs[k][share(q), :]
        for p in mates:
            arrived(cr[k].at[p], c_r.at[k, p])
            total = total + cr[k][p]
        pr[:, cols(k)] = total
        truth = tg[:, cols(k)]
        for at, value in enumerate((total * truth, total * total, truth * truth)):
            sacc[at] += lane_groups(value)
        kept = valid * total
        stats = by_slide(kept * truth) + by_slide(kept * total) + by_slide(valid * truth * truth)
        s1[q, 0 : 3 * slides, cols(k)] = jnp.concatenate(stats, axis=0)

    early = sum(forward_widths[:EARLY])
    parts = (pl.ds(0, early), pl.ds(early, genes - early))

    def sum_plane(at):
        for p in mates:
            send(s1.at[q, :, parts[at]], s1.at[q, :, parts[at]], s1_s, s1_r.at[at, q], mate(p))

    def sum_line(at):
        for p in mates:
            arrived(s1.at[p, :, parts[at]], s1_r.at[at, p])
        s2[z, :, parts[at]] = (s1[0, :, parts[at]] + s1[1, :, parts[at]]) + (s1[2, :, parts[at]] + s1[3, :, parts[at]])
        for o in others:
            send(s2.at[z, :, parts[at]], s2.at[z, :, parts[at]], s2_s, s2_r.at[at, z], (o * PLANE + q, core))

    kept = {}

    def finish_genes(at):
        for o in others:
            arrived(s2.at[o, :, parts[at]], s2_r.at[at, o])
        total = s2[0, :, parts[at]]
        for line in range(1, lines):
            total = total + s2[line, :, parts[at]]
        gene_dot, gene_pred, gene_true = total[0:2], total[2:4], total[4:6]
        gene_inv = lax.rsqrt(gene_pred * gene_true + tiny)
        cos_gene = gene_dot * gene_inv
        gv[0:2, parts[at]] = gene_inv
        gv[2:4, parts[at]] = cos_gene * gene_true / (gene_pred * gene_true + tiny)
        kept["genes", at] = jnp.sum(jnp.sum(cos_gene, axis=1, keepdims=True), axis=0, keepdims=True)
        if at == 0:
            kept["mass"] = jnp.where(first, total[6:7, 0:1], total[6:7, 1:2])
            kept["cells"] = jnp.where(first, total[6:7, 2:3], total[6:7, 3:4])

    def sum_cores():
        sums = [jnp.sum(sacc[at], axis=1, keepdims=True) for at in range(3)]
        ss[core] = jnp.where(wide == 0, sums[0], jnp.where(wide == 1, sums[1], sums[2]))
        send(ss.at[core], ss.at[core], ss_s, ss_r, sibling)

    def finish_spots():
        arrived(ss.at[1 - core], ss_r)
        spot = ss[0] + ss[1]
        spot_dot, spot_pred, spot_true = spot[:, 0:1], spot[:, 1:2], spot[:, 2:3]
        spot_inv = lax.rsqrt(spot_pred * spot_true + tiny)
        cos_spot = spot_dot * spot_inv
        kept["inverse"], kept["cos"] = spot_inv, cos_spot
        kept["back"] = cos_spot * spot_true / (spot_pred * spot_true + tiny)
        sacc[0] = jnp.zeros_like(sacc[0])

    def send_grad(k):
        spot_inv, spot_back = kept["inverse"], kept["back"]
        pieces = []
        for m in range(slides):
            lo, hi = m * slide_rows, (m + 1) * slide_rows
            truth, guess = tg[lo:hi, turn_cols(k)], pr[lo:hi, turn_cols(k)]
            inverse, back = gv[m : m + 1, turn_cols(k)], gv[2 + m : 3 + m, turn_cols(k)]
            pieces.append(
                -valid[lo:hi]
                * (truth * (inverse + spot_inv[lo:hi]) - guess * back - guess * spot_back[lo:hi])
            )
        grad = jnp.concatenate(pieces, axis=0)
        here = ds[k].at[share(q)]
        here[...] = grad
        for p in mates:
            send(here, here, d_s.at[k], d_r.at[k, q], mate(p))
        sacc[0] += lane_groups(grad * pr[:, turn_cols(k)])

    def send_terms():
        mass_total, cell_total = kept["mass"], kept["cells"]
        portion = kcell / cell_total
        kl_rows = portion * (jnp.log(counted) - jnp.log(cell_total) - jnp.log(mass) + jnp.log(mass_total))
        dmass = scale_count * valid * (1.0 / mass_total - portion / mass)
        terms = jnp.sum(scale_count * kl_rows - valid * kept["cos"], axis=0, keepdims=True)
        l1[q] = jnp.broadcast_to(terms, (8, LANES))
        for p in mates:
            send(l1.at[q], l1.at[q], l1_s, l1_r.at[q], mate(p))
        inner = jnp.sum(sacc[0], axis=1, keepdims=True)
        inn[core] = jnp.where(wide == 0, inner, kept["genes", 0] + kept["genes", 1])
        send(inn.at[core], inn.at[core], in_s, in_r, sibling)
        rowv[1] = jnp.broadcast_to(dmass, (rows, LANES))

    middle = lines // 2

    def backward_product(k):
        for p in mates:
            arrived(ds[k].at[share(p)], d_r.at[k, p])
        value = ds[k][...]
        factor = threefold(value, 0, True)
        grad_3[:, three_turn_cols(k)] = threefold(value, 1, False)
        if not halved(k):
            es[k][...] = product(turned_3[...], factor, ((1,), (0,)))

        for turn in range(2):
            if halved(k):
                side = (1 - z // middle) if turn == 0 else z // middle
                pair = pl.ds(pl.multiple_of(side * middle * cb, middle * cb), middle * cb)
                es[k][pair, :] = product(turned_3[pair, :], factor, ((1,), (0,)))

            @pl.when(z == 0)
            def _():
                if halved(k):
                    pass_up(k, middle if turn == 0 else 1, middle if turn == 0 else middle - 1, turn)
                elif whole(k):
                    if turn == 0:
                        pass_up(k, 1, last, 0)
                elif turn == 0:
                    for line in range(last, 0, -1):
                        pass_up(k, line, 1, line)

            @pl.when(z == last)
            def _():
                if halved(k):
                    pass_down(k, 0 if turn == 0 else middle, middle if turn == 0 else middle - 1, turn)
                elif whole(k):
                    if turn == 0:
                        pass_down(k, 0, last, 0)
                elif turn == 0:
                    for line in range(last):
                        pass_down(k, line, 1, line)

    def halved(k):
        return k == 0

    def whole(k):
        return 0 < k < turns - SPLIT

    def pass_up(k, line, count, slot):
        here = pl.ds(line * cb, count * cb)
        send(es[k].at[here], ru[k].at[here], ru_s.at[k], ru_r.at[k, slot], up)

    def pass_down(k, line, count, slot):
        here = pl.ds(line * cb, count * cb)
        send(es[k].at[here], rd[k].at[here], rd_s.at[k], rd_r.at[k, slot], down)

    def take_up(k, line, count, slot):
        arrived(ru[k].at[pl.ds(line * cb, count * cb)], ru_r.at[k, slot])

    def take_down(k, line, count, slot):
        arrived(rd[k].at[pl.ds(line * cb, count * cb)], rd_r.at[k, slot])

    def add_up(k, line, count):
        here = pl.ds(line * cb, count * cb)
        es[k][here, :] += ru[k][here, :]

    def add_down(k, line, count):
        here = pl.ds(line * cb, count * cb)
        es[k][here, :] += rd[k][here, :]

    def rising(k, at):
        if halved(k) or whole(k):
            start = middle if halved(k) else at
            take_up(k, start, lines - start, 0)
            above = max(at + 1, start)
            add_up(k, above, lines - above)
            pass_up(k, above, lines - above, 0)
        else:
            for line in range(last, at, -1):
                take_up(k, line, 1, line)
                add_up(k, line, 1)
                pass_up(k, line, 1, line)

    def falling(k, at):
        if halved(k) or whole(k):
            end = middle if halved(k) else at + 1
            take_down(k, 0, end, 0)
            below = min(at, end)
            add_down(k, 0, below)
            pass_down(k, 0, below, 0)
        else:
            for line in range(at):
                take_down(k, line, 1, line)
                add_down(k, line, 1)
                pass_down(k, line, 1, line)

    def add_near(k):
        for at in range(1, last):

            @pl.when(z == at)
            def _():
                (rising if low(at) else falling)(k, at)

    def add_far(k):
        for at in range(1, last):

            @pl.when(z == at)
            def _():
                (falling if low(at) else rising)(k, at)

    def finish_expr(k):
        for at in range(lines):

            @pl.when(z == at)
            def _():
                own = pl.ds(at * cb, cb)
                total = es[k][own, :]
                if at > 0:
                    if halved(k) and at < middle:
                        take_up(k, at, 1, 1)
                    elif at == last and (halved(k) or whole(k)):
                        take_up(k, at, 1, 0)
                    elif not halved(k) and not whole(k):
                        take_up(k, at, 1, at)
                    total = total + ru[k][own, :]
                if at < last:
                    if halved(k) and at >= middle:
                        take_down(k, at, 1, 1)
                    elif at == 0 and (halved(k) or whole(k)):
                        take_down(k, at, 1, 0)
                    elif not halved(k) and not whole(k):
                        take_down(k, at, 1, at)
                    total = total + rd[k][own, :]
                ge[:, turn_cols(k)] = total

    def probs_gradient(k):
        at = three_turn_cols(k)
        part = product(grad_3[:, at], expr_3[:, at], ((1,), (1,)))
        if k == 0:
            fs[...] = part
        else:
            fs[...] += part

    def slide_of(p, m):
        return pl.ds(pl.multiple_of(p * rows + m * slide_rows, slide_rows), slide_rows)

    def sum_probs_cores():
        for p in mates + (q,):
            fx[p] = fs[slide_of(p, 1 - core), :]
            send(fx.at[p], fy.at[p], fx_s, fx_r.at[p], sibling)

    def return_probs():
        for p in mates + (q,):
            arrived(fy.at[p], fx_r.at[p])
            fz[p] = fs[slide_of(p, core), :] + fy[p]
        for p in mates:
            send(fz.at[p], fr.at[q], f_s, f_r.at[q], mate(p))
        fr[q] = fz[q]

    def pass_terms():
        for p in mates:
            arrived(l1.at[p], l1_r.at[p])
        l2[z] = (l1[0] + l1[1]) + (l1[2] + l1[3])
        for o in others:
            send(l2.at[z], l2.at[z], l2_s, l2_r.at[z], (o * PLANE + q, core))

    def part_of(slide, m):
        start = slide * slide_rows + m * (slide_rows // 2)
        return pl.ds(pl.multiple_of(start, slide_rows // 2), slide_rows // 2)

    def finish_logits():
        arrived(inn.at[1 - core], in_r)
        rowv[2] = (inn[0] + inn[1]) + rowv[1] * rowv[0]
        for p in mates:
            arrived(fr.at[p], f_r.at[p])
        for m in range(2):

            @pl.loop(0, slide_rows // STEP_ROWS // 2)
            def _(step):
                row_at = (m * (slide_rows // STEP_ROWS // 2) + step) * STEP_ROWS
                at = pl.ds(pl.multiple_of(row_at, STEP_ROWS), STEP_ROWS)
                whole_at = pl.ds(pl.multiple_of(core * slide_rows + row_at, STEP_ROWS), STEP_ROWS)
                by_mass, total_inner = rowv[1, whole_at, 0:1], rowv[2, whole_at, 0:1]
                for p in range(PLANE):
                    for line in range(lines):
                        here, there = pl.ds(line * cb, cb), (line * PLANE + p) * cb
                        grad = fr[p, at, here] + by_mass * weights[:, there : there + cb]
                        glog[whole_at, pl.ds(there, cb)] = pq[p, whole_at, here] * (grad - total_inner)

            here = part_of(core, m)
            send(glog.at[here], glog.at[here], go_s, go_r.at[m], sibling)

    steps = {
        "far": forward_far,
        "near": forward_near,
        "share": share_logits,
        "take": take_probs,
        "whole": gathered,
        "product": forward_product,
        "sum": finish_pred,
        "turn": transpose,
        "plane": sum_plane,
        "line": sum_line,
        "genes": finish_genes,
        "cores": sum_cores,
        "spots": finish_spots,
        "grad": send_grad,
        "terms": send_terms,
        "backward": backward_product,
        "probs": probs_gradient,
        "exchange": sum_probs_cores,
        "return": return_probs,
        "loss": pass_terms,
        "logits": finish_logits,
        "add_near": add_near,
        "add_far": add_far,
        "expr": finish_expr,
    }
    for name, *where in STEPS:
        steps[name](*where)

    for o in others:
        arrived(l2.at[o], l2_r.at[o])
    loss = l2[0]
    for line in range(1, lines):
        loss = loss + l2[line]
    loss_ref[...] = loss[0:1, 0:1] - (inn[0, 0:1, 1:2] + inn[1, 0:1, 1:2])
    for m in range(2):
        arrived(glog.at[part_of(1 - core, m)], go_r.at[m])

    for k in range(chunks):

        @pl.when(z < last)
        def _():
            sent(bb[k].at[block(z)], ou_s.at[k])

        @pl.when(z > 0)
        def _():
            sent(bb[k].at[block(z)], od_s.at[k])

        for at in range(1, last):

            @pl.when(z == at)
            def _():
                sent(bb[k].at[pl.ds(0, at * cb)], fu_s.at[k])
                sent(bb[k].at[pl.ds((at + 1) * cb, (last - at) * cb)], fd_s.at[k])

    for k in range(turns):
        for at in range(lines):

            @pl.when(z == at)
            def _():
                if at < last:
                    sent(es[k].at[pl.ds((at + 1) * cb, (last - at) * cb)], ru_s.at[k])
                if at > 0:
                    sent(es[k].at[pl.ds(0, at * cb)], rd_s.at[k])

    three = pl.ds(0, len(mates))
    sent(ab.at[three, half(0)], a_s)
    sent(ab.at[three, half(0)], a2_s)
    sent(rs.at[three], r_s)
    for k in range(chunks):
        sent(cr[k].at[three], c_s.at[k])
    sent(s1.at[three], s1_s)
    sent(s2.at[pl.ds(0, last)], s2_s)
    sent(ss.at[0], ss_s)
    for k in range(turns):
        sent(ds[k].at[pl.ds(0, len(mates) * rows)], d_s.at[k])
    sent(inn.at[0], in_s)
    sent(l1.at[three], l1_s)
    sent(l2.at[pl.ds(0, last)], l2_s)
    sent(fr.at[three], f_s)
    sent(fx, fx_s)
    sent(glog.at[half(0)], go_s)


def lane_groups(value):
    parts = [value[:, at : at + LANES] for at in range(0, value.shape[1], LANES)]
    return functools.reduce(lambda a, b: a + b, parts)


def grouped(refs, sizes):
    at = 0
    for size in sizes:
        yield refs[at : at + size]
        at += size


def deliver(pred_in, loss_in, glog_in, gexp_in, pred_ref, loss_ref, glog_ref, gexp_ref, sems):
    slides, slide_rows = pred_ref.shape[0], pred_ref.shape[1]
    copies = []
    quarter = slide_rows // 4
    for at in range(4 * slides):
        part, where = pl.ds(at * quarter, quarter), pl.ds(at % 4 * quarter, quarter)
        copies.append(pltpu.make_async_copy(glog_in.at[part], glog_ref.at[at // 4, where], sems.at[0, at]))
        copies.append(pltpu.make_async_copy(pred_in.at[part], pred_ref.at[at // 4, where], sems.at[1, at]))
        copies.append(pltpu.make_async_copy(gexp_in.at[part], gexp_ref.at[part], sems.at[2, at]))
    for copy in copies:
        copy.start()
    loss_ref[...] = loss_in[...]
    for copy in copies:
        copy.wait()


def plane_call(logits, expr, spatial, slide_spots, spot_cells, cell_prior, lines):
    slides, slide_rows, cells = logits.shape
    rows = slides * slide_rows
    cb, genes = expr.shape
    quarter = lines * cb
    spots = PLANE * rows
    chunks, turns = len(FORWARD), len(BACKWARD)
    dma = pltpu.SemaphoreType.DMA
    vmem = pltpu.VMEM
    anywhere = pl.BlockSpec(memory_space=pl.ANY)
    in_vmem = pl.BlockSpec(memory_space=pltpu.VMEM)
    scratch = [
        pltpu.SMEM((slides,), jnp.int32),
        vmem((slides, slide_rows), jnp.int32),
        vmem((1, cells), jnp.int32),
        vmem((rows, cells), F32),
        vmem((PLANE, slide_rows, quarter), F32),
        vmem((rows, genes), F32),
        vmem((cb, genes), F32),
        vmem((PLANE, rows, quarter), F32),
        vmem((PLANE, rows, quarter), F32),
        vmem((PLANE, rows, quarter), F32),
        vmem((spots, 3 * quarter), BF16),
        vmem((quarter, 3 * spots), BF16),
        vmem((quarter, 3 * genes), BF16),
        vmem((3, rows, LANES), F32),
        vmem((PLANE, 8, genes), F32),
        vmem((lines, 8, genes), F32),
        vmem((8, genes), F32),
        vmem((2, rows, LANES), F32),
        vmem((3, rows, LANES), F32),
        vmem((PLANE, 8, rows), F32),
        vmem((spots, 3 * genes), BF16),
        vmem((spots, quarter), F32),
        vmem((PLANE, slide_rows, quarter), F32),
        vmem((PLANE, slide_rows, quarter), F32),
        vmem((PLANE, slide_rows, quarter), F32),
        vmem((PLANE, slide_rows, quarter), F32),
        vmem((2, rows, LANES), F32),
        vmem((PLANE, 8, LANES), F32),
        vmem((lines, 8, LANES), F32),
        dma((2 * slides + 4,)),
        dma((chunks,)),
        dma((chunks,)),
        dma((chunks,)),
        dma((chunks,)),
        dma((chunks,)),
        dma((chunks,)),
        dma((chunks,)),
        dma((chunks,)),
        dma,
        dma((PLANE,)),
        dma,
        dma((PLANE,)),
        dma,
        dma((PLANE,)),
        dma((chunks,)),
        dma((chunks, PLANE)),
        dma,
        dma((2, PLANE)),
        dma,
        dma((2, lines)),
        dma,
        dma,
        dma((turns,)),
        dma((turns, PLANE)),
        dma((turns,)),
        dma((turns, lines)),
        dma((turns,)),
        dma((turns, lines)),
        dma,
        dma((PLANE,)),
        dma,
        dma((PLANE,)),
        dma,
        dma((2,)),
        dma,
        dma,
        dma,
        dma((PLANE,)),
        dma,
        dma((lines,)),
    ]
    for shape, widths in (
        ((quarter,), FORWARD),
        ((spots,), FORWARD),
        ((PLANE, rows), FORWARD),
        ((spots,), BACKWARD),
        ((quarter,), BACKWARD),
        ((quarter,), BACKWARD),
        ((quarter,), BACKWARD),
    ):
        scratch += [vmem(shape + (width,), F32) for width in widths]
    in_hbm = functools.partial(pltpu.with_memory_space_constraint, memory_space=pltpu.HBM)
    in_place = functools.partial(pltpu.with_memory_space_constraint, memory_space=pltpu.VMEM)
    results = pl.pallas_call(
        functools.partial(plane_kernel, lines, FORWARD, BACKWARD),
        out_shape=(
            vmem((rows, genes), F32),
            jax.ShapeDtypeStruct((1, 1), F32),
            vmem((rows, cells), F32),
            vmem((cb, genes), F32),
        ),
        in_specs=[anywhere] * 6,
        out_specs=(in_vmem,) * 4,
        scratch_shapes=scratch,
        compiler_params=pltpu.CompilerParams(
            collective_id=0, has_side_effects=True, vmem_limit_bytes=48 * 1024 * 1024
        ),
    )(*map(in_hbm, (logits, expr, spatial, slide_spots, spot_cells, cell_prior.reshape(1, cells))))
    pred, loss, grad_logits, grad_expr = pl.pallas_call(
        deliver,
        out_shape=(
            jax.ShapeDtypeStruct((slides, slide_rows, genes), F32),
            jax.ShapeDtypeStruct((1, 1), F32),
            jax.ShapeDtypeStruct((slides, slide_rows, cells), F32),
            jax.ShapeDtypeStruct((cb, genes), F32),
        ),
        in_specs=[anywhere, in_vmem, anywhere, anywhere],
        out_specs=(anywhere, in_vmem, anywhere, anywhere),
        scratch_shapes=[dma((3, 4 * slides))],
        compiler_params=pltpu.CompilerParams(vmem_limit_bytes=4 * 1024 * 1024),
    )(in_place(results[0]), results[1], in_place(results[2]), in_place(results[3]))
    return pred, loss.reshape(()), grad_logits, grad_expr


def general_plan(logits, expr, spatial, slide_spots, spot_cells, cell_prior):
    place = lax.axis_index("spot")
    side = lax.axis_index("gene")
    rows_all = logits.shape[1]
    cell_rows = expr.shape[0]
    weights = cell_prior.astype(jnp.float32) / fixed_point
    gene_share = (place == 0).astype(jnp.float32)
    row_share = (side == 0).astype(jnp.float32)
    own_weights = lax.dynamic_slice_in_dim(weights, place * cell_rows, cell_rows, 0)
    expr_acc = jnp.zeros((cell_rows, expr.shape[1]), jnp.float32)
    loss_local = jnp.zeros((), jnp.float32)
    pred_list = []
    grad_list = []
    for slide in range(logits.shape[0]):
        logit_rows = logits[slide]
        counted = spot_cells[slide].astype(jnp.float32)
        target = spatial[slide]
        positions = place * rows_all + jnp.arange(rows_all, dtype=jnp.int32)
        valid = (positions < slide_spots[slide]).astype(jnp.float32)
        peak = jnp.max(logit_rows, axis=1, keepdims=True)
        raised = jnp.exp(logit_rows - peak)
        probs = raised / jnp.sum(raised, axis=1, keepdims=True)
        mass = jnp.dot(probs, weights, precision=lax.Precision.HIGHEST)
        blocks = lax.all_to_all(probs, "spot", split_axis=1, concat_axis=0, tiled=True)
        pred = lax.psum_scatter(
            jnp.dot(blocks, expr, precision=lax.Precision.HIGHEST),
            "spot",
            scatter_dimension=0,
            tiled=True,
        )
        gene_dot = jnp.sum(valid[:, None] * pred * target, axis=0)
        gene_pred = jnp.sum(valid[:, None] * pred * pred, axis=0)
        gene_true = jnp.sum(valid[:, None] * target * target, axis=0)
        mass_part = jnp.sum(valid * mass)
        kcell = valid * counted
        cell_part = jnp.sum(kcell)
        spot_dot = jnp.sum(pred * target, axis=1)
        spot_pred = jnp.sum(pred * pred, axis=1)
        spot_true = jnp.sum(target * target, axis=1)
        gene_dot, gene_pred, gene_true, mass_total, cell_total = lax.psum(
            (gene_dot, gene_pred, gene_true, mass_part, cell_part), "spot"
        )
        spot_dot, spot_pred, spot_true = lax.psum((spot_dot, spot_pred, spot_true), "gene")
        gene_inv = lax.rsqrt(gene_pred * gene_true + tiny)
        cos_gene = gene_dot * gene_inv
        spot_inv = lax.rsqrt(spot_pred * spot_true + tiny)
        cos_spot = spot_dot * spot_inv
        share = kcell / cell_total
        scale_count = slide_spots[slide].astype(jnp.float32)
        kl_part = jnp.sum(
            share * (jnp.log(counted) - jnp.log(cell_total) - jnp.log(mass) + jnp.log(mass_total))
        )
        loss_local = loss_local - gene_share * jnp.sum(cos_gene)
        loss_local = loss_local + row_share * (scale_count * kl_part - jnp.sum(valid * cos_spot))
        gene_back = cos_gene * gene_true / (gene_pred * gene_true + tiny)
        spot_back = cos_spot * spot_true / (spot_pred * spot_true + tiny)
        dpred = -valid[:, None] * (
            target * (gene_inv[None, :] + spot_inv[:, None])
            - pred * gene_back[None, :]
            - pred * spot_back[:, None]
        )
        dmass = scale_count * valid * (1.0 / mass_total - share / mass)
        pred_list.append(pred)
        grads_full, mass_full = (
            lax.all_gather(dpred, "spot", axis=0, tiled=True),
            lax.all_gather(dmass, "spot", axis=0, tiled=True),
        )
        dprob_cells = jnp.dot(grads_full, expr.T, precision=lax.Precision.HIGHEST)
        dprob_cells = lax.psum(dprob_cells, "gene")
        expr_acc = expr_acc + lax.dot_general(
            blocks, grads_full, (((0,), (0,)), ((), ())), precision=lax.Precision.HIGHEST
        )
        dprob_cells = dprob_cells + mass_full[:, None] * own_weights[None, :]
        dprob_rows = lax.all_to_all(dprob_cells, "spot", split_axis=0, concat_axis=1, tiled=True)
        inner = jnp.sum(probs * dprob_rows, axis=1, keepdims=True)
        dlogit = probs * (dprob_rows - inner)
        grad_list.append(dlogit)
    loss = lax.psum(loss_local, ("spot", "gene"))
    return (jnp.stack(pred_list), loss, jnp.stack(grad_list), expr_acc)


def solution(mesh):
    places = mesh.shape["spot"]

    def on_device(logits, expr, spatial, slide_spots, spot_cells, cell_prior):
        if places == PLANE * PLANE and mesh.shape["gene"] == 2 and expr.shape[1] == sum(FORWARD):
            return plane_call(
                logits, expr, spatial, slide_spots, spot_cells, cell_prior, places // PLANE
            )
        return general_plan(logits, expr, spatial, slide_spots, spot_cells, cell_prior)

    in_specs = (
        P(None, "spot", None),
        P("spot", "gene"),
        P(None, "spot", "gene"),
        P(),
        P(None, "spot"),
        P(),
    )
    out_specs = (P(None, "spot", "gene"), P(), P(None, "spot", None), P("spot", "gene"))
    return jax.shard_map(
        on_device, mesh=mesh, in_specs=in_specs, out_specs=out_specs, check_vma=False
    )
```

```python
import functools

import jax
import jax.numpy as jnp
from jax import lax
from jax.experimental import pallas as pl
from jax.experimental.pallas import tpu as pltpu
from jax.sharding import PartitionSpec as P

tiny = 1e-06
fixed_point = 16384.0
F32 = jnp.float32
BF16 = jnp.bfloat16
MESH = pl.DeviceIdType.MESH

PLANE = 4
LANES = 128
STEP_ROWS = 16
FORWARD = (256, 256, 256, 256)
BACKWARD = (128, 128, 256, 256, 256)
SPLIT = 2
LEAD = 2
EARLY = 3
STEPS = (
    ("far", 0),
    ("share",),
    ("far", 1),
    ("near", 0),
    ("take",),
    ("whole", 0),
    ("product", 0),
    ("turn", 0),
    ("whole", 1),
    ("near", 1),
    ("product", 1),
    ("far", 2),
    ("near", 2),
    ("whole", 2),
    ("product", 2),
    ("far", 3),
    ("sum", 0),
    ("sum", 1),
    ("whole", 3),
    ("near", 3),
    ("product", 3),
    ("sum", 2),
    ("plane", 0),
    ("sum", 3),
    ("plane", 1),
    ("cores",),
    ("line", 0),
    ("line", 1),
    ("spots",),
    ("genes", 0),
    ("grad", 0),
    ("grad", 1),
    ("genes", 1),
    ("grad", 2),
    ("turn", 1),
    ("backward", 0),
    ("add_near", 0),
    ("probs", 0),
    ("backward", 1),
    ("grad", 3),
    ("add_near", 1),
    ("grad", 4),
    ("add_far", 0),
    ("probs", 1),
    ("terms",),
    ("backward", 2),
    ("probs", 2),
    ("backward", 3),
    ("add_far", 1),
    ("add_near", 2),
    ("probs", 3),
    ("backward", 4),
    ("probs", 4),
    ("exchange",),
    ("add_near", 3),
    ("expr", 0),
    ("return",),
    ("loss",),
    ("expr", 1),
    ("add_far", 2),
    ("add_far", 3),
    ("add_near", 4),
    ("logits",),
    ("add_far", 4),
    ("expr", 2),
    ("expr", 3),
    ("expr", 4),
)


def halves(value):
    high = value.astype(BF16)
    return high, (value - high.astype(F32)).astype(BF16)


def threefold(value, axis, mixed):
    high, low = halves(value)
    return jnp.concatenate([high, low, high] if mixed else [high, high, low], axis=axis)


def product(a, b, contract):
    return lax.dot_general(a, b, (contract, ((), ())), preferred_element_type=F32)


def plane_kernel(lines, forward_widths, backward_widths, *refs):
    chunks, turns = len(forward_widths), len(backward_widths)
    (
        (logits_ref, expr_ref, spatial_ref, count_in, cells_in, prior_in),
        (pr, loss_ref, glog, ge),
        (count_ref, cells_ref, prior_ref, lg, lq, tg, ex, pq, ab, af, probs_3, turned_3, expr_3, sacc, s1, s2, gv, ss, rowv, rs),
        (grad_3, fs, fx, fy, fz, fr, inn, l1, l2),
        (loc, ou_s, ou_r, od_s, od_r, fu_s, fu_r, fd_s, fd_r, a_s, a_r, a2_s, a2_r, r_s, r_r),
        (c_s, c_r, s1_s, s1_r, s2_s, s2_r, ss_s, ss_r, d_s, d_r, ru_s, ru_r, rd_s, rd_r),
        (f_s, f_r, fx_s, fx_r, go_s, go_r, in_s, in_r, l1_s, l1_r, l2_s, l2_r),
        bb,
        cs,
        cr,
        ds,
        es,
        ru,
        rd,
    ) = grouped(refs, (6, 4, 20, 9, 15, 14, 12, chunks, chunks, chunks, turns, turns, turns, turns))
    place = lax.axis_index("spot")
    core = lax.axis_index("gene")
    z = place // PLANE
    q = place % PLANE
    col, row = q % 2, q // 2
    mates = ((1 - row) * 2 + 1 - col, row * 2 + 1 - col, (1 - row) * 2 + col)
    others = tuple((z + step) % lines for step in range(1, lines))
    up, down = (place + PLANE, core), (place - PLANE, core)
    sibling = (place, 1 - core)
    slides, slide_rows = logits_ref.shape[0], logits_ref.shape[1]
    rows = slides * slide_rows
    cb = expr_ref.shape[0]
    genes = expr_ref.shape[1]
    last = lines - 1

    def mate(p):
        return (z * PLANE + p, core)

    def send(src, dst, send_sem, recv_sem, device):
        copy = pltpu.make_async_remote_copy(
            src_ref=src, dst_ref=dst, send_sem=send_sem, recv_sem=recv_sem, device_id=device, device_id_type=MESH
        )
        copy.start()

    def arrived(dst, recv_sem):
        pltpu.make_async_copy(dst, dst, recv_sem).wait()

    sent = arrived

    def cols(k):
        return pl.ds(sum(forward_widths[:k]), forward_widths[k])

    def turn_cols(k):
        return pl.ds(sum(backward_widths[:k]), backward_widths[k])

    def block(index):
        return pl.ds(pl.multiple_of(index * cb, cb), cb)

    def share(index):
        return pl.ds(pl.multiple_of(index * rows, rows), rows)

    def half(index):
        return pl.ds(pl.multiple_of(index * slide_rows, slide_rows), slide_rows)

    small = ((prior_in, prior_ref), (count_in, count_ref), (cells_in, cells_ref))
    pltpu.make_async_copy(expr_ref, ex, loc.at[2 * slides]).start()
    for m in range(slides):
        pltpu.make_async_copy(logits_ref.at[m], lg.at[half(m)], loc.at[m]).start()
    for at, (src, dst) in enumerate(small):
        pltpu.make_async_copy(src, dst, loc.at[2 * slides + 1 + at]).start()
    for m in range(slides):
        pltpu.make_async_copy(spatial_ref.at[m], tg.at[half(m)], loc.at[slides + m]).start()

    barrier = pltpu.get_barrier_semaphore()
    for p in mates:
        pl.semaphore_signal(barrier, inc=1, device_id=mate(p), device_id_type=MESH)
    for o in others:
        pl.semaphore_signal(barrier, inc=1, device_id=(o * PLANE + q, core), device_id_type=MESH)
    pl.semaphore_signal(barrier, inc=1, device_id=sibling, device_id_type=MESH)
    pltpu.make_async_copy(expr_ref, ex, loc.at[2 * slides]).wait()
    for k in range(chunks):
        bb[k][block(z), :] = ex[:, cols(k)]
    for m in range(slides):
        pltpu.make_async_copy(logits_ref.at[m], lg.at[half(m)], loc.at[m]).wait()
    for p in range(PLANE):
        for line in range(lines):
            lq[p, :, pl.ds(line * cb, cb)] = lg[half(core), pl.ds((line * PLANE + p) * cb, cb)]
    pl.semaphore_wait(barrier, len(mates) + len(others) + 1)

    def own_up(k):
        here = bb[k].at[block(z)]
        send(here, here, ou_s.at[k], ou_r.at[k], up)

    def own_down(k):
        here = bb[k].at[block(z)]
        send(here, here, od_s.at[k], od_r.at[k], down)

    def low(at):
        return 2 * at < lines

    for at in range(lines):

        @pl.when(z == at)
        def _():
            for k in range(chunks):
                if at < last and (not low(at) or at == 0 or k < LEAD):
                    own_up(k)
                if at > 0 and (low(at) or at == last or k < LEAD):
                    own_down(k)

    for p in mates:
        send(lq.at[p], ab.at[q, half(core)], a_s, a_r.at[q], mate(p))

    def from_below(k, at):
        arrived(bb[k].at[pl.ds((at - 1) * cb, cb)], ou_r.at[k])
        if at > 1:
            arrived(bb[k].at[pl.ds(0, (at - 1) * cb)], fu_r.at[k])

    def from_above(k, at):
        arrived(bb[k].at[pl.ds((at + 1) * cb, cb)], od_r.at[k])
        if at < last - 1:
            arrived(bb[k].at[pl.ds((at + 2) * cb, (last - 1 - at) * cb)], fd_r.at[k])

    def upward(k, at):
        from_below(k, at)
        here = bb[k].at[pl.ds(0, at * cb)]
        send(here, here, fu_s.at[k], fu_r.at[k], up)

    def downward(k, at):
        from_above(k, at)
        here = bb[k].at[pl.ds((at + 1) * cb, (last - at) * cb)]
        send(here, here, fd_s.at[k], fd_r.at[k], down)

    def forward_far(k):
        for at in range(1, last):

            @pl.when(z == at)
            def _():
                (upward if low(at) else downward)(k, at)
                if k + LEAD < chunks:
                    (own_up if low(at) else own_down)(k + LEAD)

    def forward_near(k):
        for at in range(1, last):

            @pl.when(z == at)
            def _():
                (downward if low(at) else upward)(k, at)

    def gathered(k):
        @pl.when(z == 0)
        def _():
            from_above(k, 0)

        @pl.when(z == last)
        def _():
            from_below(k, last)

    for at, (src, dst) in enumerate(small):
        pltpu.make_async_copy(src, dst, loc.at[2 * slides + 1 + at]).wait()
    weights = prior_ref[...].astype(F32) / fixed_point

    @pl.loop(0, rows // STEP_ROWS)
    def _(step):
        at = pl.ds(pl.multiple_of(step * STEP_ROWS, STEP_ROWS), STEP_ROWS)
        value = lg[at, :]
        peak = jnp.max(value, axis=1, keepdims=True)
        raised = jnp.exp(value - peak)
        scale = 1.0 / jnp.sum(raised, axis=1, keepdims=True)
        probs = raised * scale
        mass_rows = jnp.sum(probs * weights, axis=1, keepdims=True)
        rowv[0, at, :] = jnp.broadcast_to(mass_rows, (STEP_ROWS, LANES))
        rowv[1, at, :] = jnp.broadcast_to(peak, (STEP_ROWS, LANES))
        rowv[2, at, :] = jnp.broadcast_to(scale, (STEP_ROWS, LANES))
        for p in range(PLANE):
            for line in range(lines):
                at_cells = (line * PLANE + p) * cb
                pq[p, at, pl.ds(line * cb, cb)] = probs[:, at_cells : at_cells + cb]

    wide = lax.broadcasted_iota(jnp.int32, (rows, LANES), 1)
    rs[q] = jnp.where(wide == 0, rowv[1], rowv[2]).T[0:8]
    for p in mates:
        send(rs.at[q], rs.at[q], r_s, r_r.at[q], mate(p))

    rid = lax.broadcasted_iota(jnp.int32, (rows, 1), 0)
    first = rid < slide_rows
    position = place * slide_rows + jnp.where(first, rid, rid - slide_rows)
    count = jnp.where(first, count_ref[0], count_ref[1])
    valid = (position < count).astype(F32)
    scale_count = count.astype(F32)
    square = (slide_rows, slide_rows)
    eye = lax.broadcasted_iota(jnp.int32, square, 0) == lax.broadcasted_iota(jnp.int32, square, 1)
    counted = jnp.concatenate(
        [
            jnp.sum(jnp.where(eye, cells_ref[m : m + 1, :].astype(F32), 0.0), axis=1, keepdims=True)
            for m in range(slides)
        ],
        axis=0,
    )
    mass = rowv[0, :, 0:1]
    kcell = valid * counted

    def by_slide(value):
        return [jnp.sum(value[m * slide_rows : (m + 1) * slide_rows], axis=0, keepdims=True) for m in range(slides)]

    mass_parts = by_slide(valid * mass)
    cell_parts = by_slide(kcell)
    lane = lax.broadcasted_iota(jnp.int32, (1, LANES), 1)
    scalars = jnp.zeros((1, LANES), F32)
    for at, value in enumerate(mass_parts + cell_parts):
        scalars = jnp.where(lane == at, value, scalars)
    for m in range(slides):
        pltpu.make_async_copy(spatial_ref.at[m], tg.at[half(m)], loc.at[slides + m]).wait()
    sacc[...] = jnp.zeros_like(sacc)
    s1[q, 3 * slides :, :] = jnp.zeros((8 - 3 * slides, genes), F32)
    s1[q, 3 * slides : 3 * slides + 1, 0:LANES] = scalars

    def share_logits():
        for p in (mates[1], mates[2], mates[0]):
            here = ab.at[p, half(core)]
            arrived(here, a_r.at[p])
            send(here, here, a2_s, a2_r.at[p], sibling)

    def take_probs():
        af[q] = pq[q]
        probs_3[share(q), :] = threefold(pq[q], 1, False)
        for p in (mates[1], mates[2], mates[0]):
            arrived(rs.at[p], r_r.at[p])
            arrived(ab.at[p, half(1 - core)], a2_r.at[p])
            by_row = rs[p].T
            probs = jnp.exp(ab[p] - by_row[:, 0:1]) * by_row[:, 1:2]
            af[p] = probs
            probs_3[share(p), :] = threefold(probs, 1, False)

    def transpose(part):
        for p in (2 * part, 2 * part + 1):
            high, low_part = halves(af[p].T)
            for at, value in enumerate((high, high, low_part)):
                turned_3[:, pl.ds(at * PLANE * rows + p * rows, rows)] = value

    def keep_expr(k, value):
        start = sum(forward_widths[:k])
        for turn in range(turns):
            origin, width = sum(backward_widths[:turn]), backward_widths[turn]
            lo, hi = max(start, origin), min(start + forward_widths[k], origin + width)
            if lo < hi:
                high, low_part = halves(value[:, lo - start : hi - start])
                for at, part in enumerate((high, low_part, high)):
                    expr_3[:, pl.ds(3 * origin + at * width + lo - origin, hi - lo)] = part

    def three_turn_cols(k):
        return pl.ds(3 * sum(backward_widths[:k]), 3 * backward_widths[k])

    def forward_product(k):
        value = bb[k][...]
        factor = threefold(value, 0, True)
        keep_expr(k, value)
        if k < chunks - 1:
            cs[k][...] = product(probs_3[...], factor, ((1,), (0,)))
            for p in mates:
                pass_pred(k, p)
        else:
            for side, served in ((1 - row, (mates[0], mates[2])), (row, (mates[1],))):
                pair = pl.ds(pl.multiple_of(2 * side * rows, 2 * rows), 2 * rows)
                cs[k][pair, :] = product(probs_3[pair, :], factor, ((1,), (0,)))
                for p in served:
                    pass_pred(k, p)

    def pass_pred(k, p):
        send(cs[k].at[share(p)], cr[k].at[q], c_s.at[k], c_r.at[k, q], mate(p))

    def finish_pred(k):
        total = cs[k][share(q), :]
        for p in mates:
            arrived(cr[k].at[p], c_r.at[k, p])
            total = total + cr[k][p]
        pr[:, cols(k)] = total
        truth = tg[:, cols(k)]
        for at, value in enumerate((total * truth, total * total, truth * truth)):
            sacc[at] += lane_groups(value)
        kept = valid * total
        stats = by_slide(kept * truth) + by_slide(kept * total) + by_slide(valid * truth * truth)
        s1[q, 0 : 3 * slides, cols(k)] = jnp.concatenate(stats, axis=0)

    early = sum(forward_widths[:EARLY])
    parts = (pl.ds(0, early), pl.ds(early, genes - early))

    def sum_plane(at):
        for p in mates:
            send(s1.at[q, :, parts[at]], s1.at[q, :, parts[at]], s1_s, s1_r.at[at, q], mate(p))

    def sum_line(at):
        for p in mates:
            arrived(s1.at[p, :, parts[at]], s1_r.at[at, p])
        s2[z, :, parts[at]] = (s1[0, :, parts[at]] + s1[1, :, parts[at]]) + (s1[2, :, parts[at]] + s1[3, :, parts[at]])
        for o in others:
            send(s2.at[z, :, parts[at]], s2.at[z, :, parts[at]], s2_s, s2_r.at[at, z], (o * PLANE + q, core))

    kept = {}

    def finish_genes(at):
        for o in others:
            arrived(s2.at[o, :, parts[at]], s2_r.at[at, o])
        total = s2[0, :, parts[at]]
        for line in range(1, lines):
            total = total + s2[line, :, parts[at]]
        gene_dot, gene_pred, gene_true = total[0:2], total[2:4], total[4:6]
        gene_inv = lax.rsqrt(gene_pred * gene_true + tiny)
        cos_gene = gene_dot * gene_inv
        gv[0:2, parts[at]] = gene_inv
        gv[2:4, parts[at]] = cos_gene * gene_true / (gene_pred * gene_true + tiny)
        kept["genes", at] = jnp.sum(jnp.sum(cos_gene, axis=1, keepdims=True), axis=0, keepdims=True)
        if at == 0:
            kept["mass"] = jnp.where(first, total[6:7, 0:1], total[6:7, 1:2])
            kept["cells"] = jnp.where(first, total[6:7, 2:3], total[6:7, 3:4])

    def sum_cores():
        sums = [jnp.sum(sacc[at], axis=1, keepdims=True) for at in range(3)]
        ss[core] = jnp.where(wide == 0, sums[0], jnp.where(wide == 1, sums[1], sums[2]))
        send(ss.at[core], ss.at[core], ss_s, ss_r, sibling)

    def finish_spots():
        arrived(ss.at[1 - core], ss_r)
        spot = ss[0] + ss[1]
        spot_dot, spot_pred, spot_true = spot[:, 0:1], spot[:, 1:2], spot[:, 2:3]
        spot_inv = lax.rsqrt(spot_pred * spot_true + tiny)
        cos_spot = spot_dot * spot_inv
        kept["inverse"], kept["cos"] = spot_inv, cos_spot
        kept["back"] = cos_spot * spot_true / (spot_pred * spot_true + tiny)
        sacc[0] = jnp.zeros_like(sacc[0])

    def send_grad(k):
        spot_inv, spot_back = kept["inverse"], kept["back"]
        pieces = []
        for m in range(slides):
            lo, hi = m * slide_rows, (m + 1) * slide_rows
            truth, guess = tg[lo:hi, turn_cols(k)], pr[lo:hi, turn_cols(k)]
            inverse, back = gv[m : m + 1, turn_cols(k)], gv[2 + m : 3 + m, turn_cols(k)]
            pieces.append(
                -valid[lo:hi]
                * (truth * (inverse + spot_inv[lo:hi]) - guess * back - guess * spot_back[lo:hi])
            )
        grad = jnp.concatenate(pieces, axis=0)
        here = ds[k].at[share(q)]
        here[...] = grad
        for p in mates:
            send(here, here, d_s.at[k], d_r.at[k, q], mate(p))
        sacc[0] += lane_groups(grad * pr[:, turn_cols(k)])

    def send_terms():
        mass_total, cell_total = kept["mass"], kept["cells"]
        portion = kcell / cell_total
        kl_rows = portion * (jnp.log(counted) - jnp.log(cell_total) - jnp.log(mass) + jnp.log(mass_total))
        dmass = scale_count * valid * (1.0 / mass_total - portion / mass)
        terms = jnp.sum(scale_count * kl_rows - valid * kept["cos"], axis=0, keepdims=True)
        l1[q] = jnp.broadcast_to(terms, (8, LANES))
        for p in mates:
            send(l1.at[q], l1.at[q], l1_s, l1_r.at[q], mate(p))
        inner = jnp.sum(sacc[0], axis=1, keepdims=True)
        inn[core] = jnp.where(wide == 0, inner, kept["genes", 0] + kept["genes", 1])
        send(inn.at[core], inn.at[core], in_s, in_r, sibling)
        rowv[1] = jnp.broadcast_to(dmass, (rows, LANES))

    middle = lines // 2

    def backward_product(k):
        for p in mates:
            arrived(ds[k].at[share(p)], d_r.at[k, p])
        value = ds[k][...]
        factor = threefold(value, 0, True)
        grad_3[:, three_turn_cols(k)] = threefold(value, 1, False)
        if not halved(k):
            es[k][...] = product(turned_3[...], factor, ((1,), (0,)))

        for turn in range(2):
            if halved(k):
                side = (1 - z // middle) if turn == 0 else z // middle
                pair = pl.ds(pl.multiple_of(side * middle * cb, middle * cb), middle * cb)
                es[k][pair, :] = product(turned_3[pair, :], factor, ((1,), (0,)))

            @pl.when(z == 0)
            def _():
                if halved(k):
                    pass_up(k, middle if turn == 0 else 1, middle if turn == 0 else middle - 1, turn)
                elif whole(k):
                    if turn == 0:
                        pass_up(k, 1, last, 0)
                elif turn == 0:
                    for line in range(last, 0, -1):
                        pass_up(k, line, 1, line)

            @pl.when(z == last)
            def _():
                if halved(k):
                    pass_down(k, 0 if turn == 0 else middle, middle if turn == 0 else middle - 1, turn)
                elif whole(k):
                    if turn == 0:
                        pass_down(k, 0, last, 0)
                elif turn == 0:
                    for line in range(last):
                        pass_down(k, line, 1, line)

    def halved(k):
        return k == 0

    def whole(k):
        return 0 < k < turns - SPLIT

    def pass_up(k, line, count, slot):
        here = pl.ds(line * cb, count * cb)
        send(es[k].at[here], ru[k].at[here], ru_s.at[k], ru_r.at[k, slot], up)

    def pass_down(k, line, count, slot):
        here = pl.ds(line * cb, count * cb)
        send(es[k].at[here], rd[k].at[here], rd_s.at[k], rd_r.at[k, slot], down)

    def take_up(k, line, count, slot):
        arrived(ru[k].at[pl.ds(line * cb, count * cb)], ru_r.at[k, slot])

    def take_down(k, line, count, slot):
        arrived(rd[k].at[pl.ds(line * cb, count * cb)], rd_r.at[k, slot])

    def add_up(k, line, count):
        here = pl.ds(line * cb, count * cb)
        es[k][here, :] += ru[k][here, :]

    def add_down(k, line, count):
        here = pl.ds(line * cb, count * cb)
        es[k][here, :] += rd[k][here, :]

    def rising(k, at):
        if halved(k) or whole(k):
            start = middle if halved(k) else at
            take_up(k, start, lines - start, 0)
            above = max(at + 1, start)
            add_up(k, above, lines - above)
            pass_up(k, above, lines - above, 0)
        else:
            for line in range(last, at, -1):
                take_up(k, line, 1, line)
                add_up(k, line, 1)
                pass_up(k, line, 1, line)

    def falling(k, at):
        if halved(k) or whole(k):
            end = middle if halved(k) else at + 1
            take_down(k, 0, end, 0)
            below = min(at, end)
            add_down(k, 0, below)
            pass_down(k, 0, below, 0)
        else:
            for line in range(at):
                take_down(k, line, 1, line)
                add_down(k, line, 1)
                pass_down(k, line, 1, line)

    def add_near(k):
        for at in range(1, last):

            @pl.when(z == at)
            def _():
                (rising if low(at) else falling)(k, at)

    def add_far(k):
        for at in range(1, last):

            @pl.when(z == at)
            def _():
                (falling if low(at) else rising)(k, at)

    def finish_expr(k):
        for at in range(lines):

            @pl.when(z == at)
            def _():
                own = pl.ds(at * cb, cb)
                total = es[k][own, :]
                if at > 0:
                    if halved(k) and at < middle:
                        take_up(k, at, 1, 1)
                    elif at == last and (halved(k) or whole(k)):
                        take_up(k, at, 1, 0)
                    elif not halved(k) and not whole(k):
                        take_up(k, at, 1, at)
                    total = total + ru[k][own, :]
                if at < last:
                    if halved(k) and at >= middle:
                        take_down(k, at, 1, 1)
                    elif at == 0 and (halved(k) or whole(k)):
                        take_down(k, at, 1, 0)
                    elif not halved(k) and not whole(k):
                        take_down(k, at, 1, at)
                    total = total + rd[k][own, :]
                ge[:, turn_cols(k)] = total

    def probs_gradient(k):
        at = three_turn_cols(k)
        part = product(grad_3[:, at], expr_3[:, at], ((1,), (1,)))
        if k == 0:
            fs[...] = part
        else:
            fs[...] += part

    def slide_of(p, m):
        return pl.ds(pl.multiple_of(p * rows + m * slide_rows, slide_rows), slide_rows)

    def sum_probs_cores():
        for p in mates + (q,):
            fx[p] = fs[slide_of(p, 1 - core), :]
            send(fx.at[p], fy.at[p], fx_s, fx_r.at[p], sibling)

    def return_probs():
        for p in mates:
            arrived(fy.at[p], fx_r.at[p])
            fz[p] = fs[slide_of(p, core), :] + fy[p]
            send(fz.at[p], fr.at[q], f_s, f_r.at[q], mate(p))
        arrived(fy.at[q], fx_r.at[q])
        fr[q] = fs[slide_of(q, core), :] + fy[q]

    def pass_terms():
        for p in mates:
            arrived(l1.at[p], l1_r.at[p])
        l2[z] = (l1[0] + l1[1]) + (l1[2] + l1[3])
        for o in others:
            send(l2.at[z], l2.at[z], l2_s, l2_r.at[z], (o * PLANE + q, core))

    def part_of(slide, m):
        start = slide * slide_rows + m * (slide_rows // 2)
        return pl.ds(pl.multiple_of(start, slide_rows // 2), slide_rows // 2)

    def finish_logits():
        arrived(inn.at[1 - core], in_r)
        rowv[2] = (inn[0] + inn[1]) + rowv[1] * rowv[0]
        for p in mates:
            arrived(fr.at[p], f_r.at[p])
        for m in range(2):

            @pl.loop(0, slide_rows // STEP_ROWS // 2)
            def _(step):
                row_at = (m * (slide_rows // STEP_ROWS // 2) + step) * STEP_ROWS
                at = pl.ds(pl.multiple_of(row_at, STEP_ROWS), STEP_ROWS)
                whole_at = pl.ds(pl.multiple_of(core * slide_rows + row_at, STEP_ROWS), STEP_ROWS)
                by_mass, total_inner = rowv[1, whole_at, 0:1], rowv[2, whole_at, 0:1]
                for p in range(PLANE):
                    for line in range(lines):
                        here, there = pl.ds(line * cb, cb), (line * PLANE + p) * cb
                        grad = fr[p, at, here] + by_mass * weights[:, there : there + cb]
                        glog[whole_at, pl.ds(there, cb)] = pq[p, whole_at, here] * (grad - total_inner)

            here = part_of(core, m)
            send(glog.at[here], glog.at[here], go_s, go_r.at[m], sibling)

    steps = {
        "far": forward_far,
        "near": forward_near,
        "share": share_logits,
        "take": take_probs,
        "whole": gathered,
        "product": forward_product,
        "sum": finish_pred,
        "turn": transpose,
        "plane": sum_plane,
        "line": sum_line,
        "genes": finish_genes,
        "cores": sum_cores,
        "spots": finish_spots,
        "grad": send_grad,
        "terms": send_terms,
        "backward": backward_product,
        "probs": probs_gradient,
        "exchange": sum_probs_cores,
        "return": return_probs,
        "loss": pass_terms,
        "logits": finish_logits,
        "add_near": add_near,
        "add_far": add_far,
        "expr": finish_expr,
    }
    for name, *where in STEPS:
        steps[name](*where)

    for o in others:
        arrived(l2.at[o], l2_r.at[o])
    loss = l2[0]
    for line in range(1, lines):
        loss = loss + l2[line]
    loss_ref[...] = loss[0:1, 0:1] - (inn[0, 0:1, 1:2] + inn[1, 0:1, 1:2])
    for m in range(2):
        arrived(glog.at[part_of(1 - core, m)], go_r.at[m])

    for k in range(chunks):

        @pl.when(z < last)
        def _():
            sent(bb[k].at[block(z)], ou_s.at[k])

        @pl.when(z > 0)
        def _():
            sent(bb[k].at[block(z)], od_s.at[k])

        for at in range(1, last):

            @pl.when(z == at)
            def _():
                sent(bb[k].at[pl.ds(0, at * cb)], fu_s.at[k])
                sent(bb[k].at[pl.ds((at + 1) * cb, (last - at) * cb)], fd_s.at[k])

    for k in range(turns):
        for at in range(lines):

            @pl.when(z == at)
            def _():
                if at < last:
                    sent(es[k].at[pl.ds((at + 1) * cb, (last - at) * cb)], ru_s.at[k])
                if at > 0:
                    sent(es[k].at[pl.ds(0, at * cb)], rd_s.at[k])

    three = pl.ds(0, len(mates))
    sent(ab.at[three, half(0)], a_s)
    sent(ab.at[three, half(0)], a2_s)
    sent(rs.at[three], r_s)
    for k in range(chunks):
        sent(cr[k].at[three], c_s.at[k])
    sent(s1.at[three], s1_s)
    sent(s2.at[pl.ds(0, last)], s2_s)
    sent(ss.at[0], ss_s)
    for k in range(turns):
        sent(ds[k].at[pl.ds(0, len(mates) * rows)], d_s.at[k])
    sent(inn.at[0], in_s)
    sent(l1.at[three], l1_s)
    sent(l2.at[pl.ds(0, last)], l2_s)
    sent(fr.at[three], f_s)
    sent(fx, fx_s)
    sent(glog.at[half(0)], go_s)


def lane_groups(value):
    parts = [value[:, at : at + LANES] for at in range(0, value.shape[1], LANES)]
    return functools.reduce(lambda a, b: a + b, parts)


def grouped(refs, sizes):
    at = 0
    for size in sizes:
        yield refs[at : at + size]
        at += size


def plane_call(logits, expr, spatial, slide_spots, spot_cells, cell_prior, lines):
    slides, slide_rows, cells = logits.shape
    rows = slides * slide_rows
    cb, genes = expr.shape
    quarter = lines * cb
    spots = PLANE * rows
    chunks, turns = len(FORWARD), len(BACKWARD)
    dma = pltpu.SemaphoreType.DMA
    vmem = pltpu.VMEM
    anywhere = pl.BlockSpec(memory_space=pl.ANY)
    in_vmem = pl.BlockSpec(memory_space=pltpu.VMEM)
    scratch = [
        pltpu.SMEM((slides,), jnp.int32),
        vmem((slides, slide_rows), jnp.int32),
        vmem((1, cells), jnp.int32),
        vmem((rows, cells), F32),
        vmem((PLANE, slide_rows, quarter), F32),
        vmem((rows, genes), F32),
        vmem((cb, genes), F32),
        vmem((PLANE, rows, quarter), F32),
        vmem((PLANE, rows, quarter), F32),
        vmem((PLANE, rows, quarter), F32),
        vmem((spots, 3 * quarter), BF16),
        vmem((quarter, 3 * spots), BF16),
        vmem((quarter, 3 * genes), BF16),
        vmem((3, rows, LANES), F32),
        vmem((PLANE, 8, genes), F32),
        vmem((lines, 8, genes), F32),
        vmem((8, genes), F32),
        vmem((2, rows, LANES), F32),
        vmem((3, rows, LANES), F32),
        vmem((PLANE, 8, rows), F32),
        vmem((spots, 3 * genes), BF16),
        vmem((spots, quarter), F32),
        vmem((PLANE, slide_rows, quarter), F32),
        vmem((PLANE, slide_rows, quarter), F32),
        vmem((PLANE, slide_rows, quarter), F32),
        vmem((PLANE, slide_rows, quarter), F32),
        vmem((2, rows, LANES), F32),
        vmem((PLANE, 8, LANES), F32),
        vmem((lines, 8, LANES), F32),
        dma((2 * slides + 4,)),
        dma((chunks,)),
        dma((chunks,)),
        dma((chunks,)),
        dma((chunks,)),
        dma((chunks,)),
        dma((chunks,)),
        dma((chunks,)),
        dma((chunks,)),
        dma,
        dma((PLANE,)),
        dma,
        dma((PLANE,)),
        dma,
        dma((PLANE,)),
        dma((chunks,)),
        dma((chunks, PLANE)),
        dma,
        dma((2, PLANE)),
        dma,
        dma((2, lines)),
        dma,
        dma,
        dma((turns,)),
        dma((turns, PLANE)),
        dma((turns,)),
        dma((turns, lines)),
        dma((turns,)),
        dma((turns, lines)),
        dma,
        dma((PLANE,)),
        dma,
        dma((PLANE,)),
        dma,
        dma((2,)),
        dma,
        dma,
        dma,
        dma((PLANE,)),
        dma,
        dma((lines,)),
    ]
    for shape, widths in (
        ((quarter,), FORWARD),
        ((spots,), FORWARD),
        ((PLANE, rows), FORWARD),
        ((spots,), BACKWARD),
        ((quarter,), BACKWARD),
        ((quarter,), BACKWARD),
        ((quarter,), BACKWARD),
    ):
        scratch += [vmem(shape + (width,), F32) for width in widths]
    in_hbm = functools.partial(pltpu.with_memory_space_constraint, memory_space=pltpu.HBM)
    results = pl.pallas_call(
        functools.partial(plane_kernel, lines, FORWARD, BACKWARD),
        out_shape=(
            vmem((rows, genes), F32),
            jax.ShapeDtypeStruct((1, 1), F32),
            vmem((rows, cells), F32),
            vmem((cb, genes), F32),
        ),
        in_specs=[anywhere] * 6,
        out_specs=(in_vmem,) * 4,
        scratch_shapes=scratch,
        compiler_params=pltpu.CompilerParams(
            collective_id=0, has_side_effects=True, vmem_limit_bytes=48 * 1024 * 1024
        ),
    )(*map(in_hbm, (logits, expr, spatial, slide_spots, spot_cells, cell_prior.reshape(1, cells))))
    pred, loss, grad_logits, grad_expr = results
    pred = pred.reshape(slides, slide_rows, genes)
    grad_logits = grad_logits.reshape(slides, slide_rows, cells)
    return pred, loss.reshape(()), grad_logits, grad_expr


def general_plan(logits, expr, spatial, slide_spots, spot_cells, cell_prior):
    place = lax.axis_index("spot")
    side = lax.axis_index("gene")
    rows_all = logits.shape[1]
    cell_rows = expr.shape[0]
    weights = cell_prior.astype(jnp.float32) / fixed_point
    gene_share = (place == 0).astype(jnp.float32)
    row_share = (side == 0).astype(jnp.float32)
    own_weights = lax.dynamic_slice_in_dim(weights, place * cell_rows, cell_rows, 0)
    expr_acc = jnp.zeros((cell_rows, expr.shape[1]), jnp.float32)
    loss_local = jnp.zeros((), jnp.float32)
    pred_list = []
    grad_list = []
    for slide in range(logits.shape[0]):
        logit_rows = logits[slide]
        counted = spot_cells[slide].astype(jnp.float32)
        target = spatial[slide]
        positions = place * rows_all + jnp.arange(rows_all, dtype=jnp.int32)
        valid = (positions < slide_spots[slide]).astype(jnp.float32)
        peak = jnp.max(logit_rows, axis=1, keepdims=True)
        raised = jnp.exp(logit_rows - peak)
        probs = raised / jnp.sum(raised, axis=1, keepdims=True)
        mass = jnp.dot(probs, weights, precision=lax.Precision.HIGHEST)
        blocks = lax.all_to_all(probs, "spot", split_axis=1, concat_axis=0, tiled=True)
        pred = lax.psum_scatter(
            jnp.dot(blocks, expr, precision=lax.Precision.HIGHEST),
            "spot",
            scatter_dimension=0,
            tiled=True,
        )
        gene_dot = jnp.sum(valid[:, None] * pred * target, axis=0)
        gene_pred = jnp.sum(valid[:, None] * pred * pred, axis=0)
        gene_true = jnp.sum(valid[:, None] * target * target, axis=0)
        mass_part = jnp.sum(valid * mass)
        kcell = valid * counted
        cell_part = jnp.sum(kcell)
        spot_dot = jnp.sum(pred * target, axis=1)
        spot_pred = jnp.sum(pred * pred, axis=1)
        spot_true = jnp.sum(target * target, axis=1)
        gene_dot, gene_pred, gene_true, mass_total, cell_total = lax.psum(
            (gene_dot, gene_pred, gene_true, mass_part, cell_part), "spot"
        )
        spot_dot, spot_pred, spot_true = lax.psum((spot_dot, spot_pred, spot_true), "gene")
        gene_inv = lax.rsqrt(gene_pred * gene_true + tiny)
        cos_gene = gene_dot * gene_inv
        spot_inv = lax.rsqrt(spot_pred * spot_true + tiny)
        cos_spot = spot_dot * spot_inv
        share = kcell / cell_total
        scale_count = slide_spots[slide].astype(jnp.float32)
        kl_part = jnp.sum(
            share * (jnp.log(counted) - jnp.log(cell_total) - jnp.log(mass) + jnp.log(mass_total))
        )
        loss_local = loss_local - gene_share * jnp.sum(cos_gene)
        loss_local = loss_local + row_share * (scale_count * kl_part - jnp.sum(valid * cos_spot))
        gene_back = cos_gene * gene_true / (gene_pred * gene_true + tiny)
        spot_back = cos_spot * spot_true / (spot_pred * spot_true + tiny)
        dpred = -valid[:, None] * (
            target * (gene_inv[None, :] + spot_inv[:, None])
            - pred * gene_back[None, :]
            - pred * spot_back[:, None]
        )
        dmass = scale_count * valid * (1.0 / mass_total - share / mass)
        pred_list.append(pred)
        grads_full, mass_full = (
            lax.all_gather(dpred, "spot", axis=0, tiled=True),
            lax.all_gather(dmass, "spot", axis=0, tiled=True),
        )
        dprob_cells = jnp.dot(grads_full, expr.T, precision=lax.Precision.HIGHEST)
        dprob_cells = lax.psum(dprob_cells, "gene")
        expr_acc = expr_acc + lax.dot_general(
            blocks, grads_full, (((0,), (0,)), ((), ())), precision=lax.Precision.HIGHEST
        )
        dprob_cells = dprob_cells + mass_full[:, None] * own_weights[None, :]
        dprob_rows = lax.all_to_all(dprob_cells, "spot", split_axis=0, concat_axis=1, tiled=True)
        inner = jnp.sum(probs * dprob_rows, axis=1, keepdims=True)
        dlogit = probs * (dprob_rows - inner)
        grad_list.append(dlogit)
    loss = lax.psum(loss_local, ("spot", "gene"))
    return (jnp.stack(pred_list), loss, jnp.stack(grad_list), expr_acc)


def solution(mesh):
    places = mesh.shape["spot"]

    def on_device(logits, expr, spatial, slide_spots, spot_cells, cell_prior):
        if places == PLANE * PLANE and mesh.shape["gene"] == 2 and expr.shape[1] == sum(FORWARD):
            return plane_call(
                logits, expr, spatial, slide_spots, spot_cells, cell_prior, places // PLANE
            )
        return general_plan(logits, expr, spatial, slide_spots, spot_cells, cell_prior)

    in_specs = (
        P(None, "spot", None),
        P("spot", "gene"),
        P(None, "spot", "gene"),
        P(),
        P(None, "spot"),
        P(),
    )
    out_specs = (P(None, "spot", "gene"), P(), P(None, "spot", None), P("spot", "gene"))
    return jax.shard_map(
        on_device, mesh=mesh, in_specs=in_specs, out_specs=out_specs, check_vma=False
    )
```

```python
import functools

import jax
import jax.numpy as jnp
from jax import lax
from jax.experimental import pallas as pl
from jax.experimental.pallas import tpu as pltpu
from jax.sharding import PartitionSpec as P

tiny = 1e-06
fixed_point = 16384.0
F32 = jnp.float32
BF16 = jnp.bfloat16
MESH = pl.DeviceIdType.MESH

PLANE = 4
LANES = 128
STEP_ROWS = 16
FORWARD = (256, 256, 256, 256)
BACKWARD = (128, 128, 256, 256, 256)
SPLIT = 2
LEAD = 2
EARLY = 3
STEPS = (
    ("far", 0),
    ("far", 1),
    ("share",),
    ("near", 0),
    ("take",),
    ("whole", 0),
    ("product", 0),
    ("whole", 1),
    ("near", 1),
    ("product", 1),
    ("far", 2),
    ("far", 3),
    ("sum", 0),
    ("near", 2),
    ("whole", 2),
    ("product", 2),
    ("sum", 1),
    ("near", 3),
    ("whole", 3),
    ("product", 3),
    ("sum", 2),
    ("plane", 0),
    ("sum", 3),
    ("plane", 1),
    ("cores",),
    ("line", 0),
    ("spots",),
    ("genes", 0),
    ("grad", 0),
    ("grad", 1),
    ("turn", 0),
    ("grad", 2),
    ("line", 1),
    ("grad", 3),
    ("turn", 1),
    ("genes", 1),
    ("backward", 0),
    ("backward", 1),
    ("probs", 0),
    ("grad", 4),
    ("probs", 1),
    ("backward", 2),
    ("probs", 2),
    ("terms",),
    ("add_near", 0),
    ("backward", 3),
    ("add_near", 1),
    ("add_far", 0),
    ("probs", 3),
    ("add_near", 2),
    ("backward", 4),
    ("probs", 4),
    ("exchange",),
    ("add_far", 1),
    ("add_near", 3),
    ("return",),
    ("loss",),
    ("add_far", 2),
    ("expr", 0),
    ("expr", 1),
    ("add_far", 3),
    ("add_near", 4),
    ("expr", 2),
    ("expr", 3),
    ("add_far", 4),
    ("logits",),
    ("expr", 4),
)


def halves(value):
    high = value.astype(BF16)
    return high, (value - high.astype(F32)).astype(BF16)


def threefold(value, axis, mixed):
    high, low = halves(value)
    return jnp.concatenate([high, low, high] if mixed else [high, high, low], axis=axis)


def product(a, b, contract):
    return lax.dot_general(a, b, (contract, ((), ())), preferred_element_type=F32)


def plane_kernel(lines, forward_widths, backward_widths, *refs):
    chunks, turns = len(forward_widths), len(backward_widths)
    (
        (logits_ref, expr_ref, spatial_ref, count_in, cells_in, prior_in),
        (pr, loss_ref, glog, ge),
        (count_ref, cells_ref, prior_ref, lg, lq, tg, ex, pq, ab, af, probs_3, turned_3, expr_3, sacc, s1, s2, gv, ss, rowv, rs),
        (grad_3, fs, fx, fy, fz, fr, inn, l1, l2),
        (loc, ou_s, ou_r, od_s, od_r, fu_s, fu_r, fd_s, fd_r, a_s, a_r, a2_s, a2_r, r_s, r_r),
        (c_s, c_r, s1_s, s1_r, s2_s, s2_r, ss_s, ss_r, d_s, d_r, ru_s, ru_r, rd_s, rd_r),
        (f_s, f_r, fx_s, fx_r, go_s, go_r, in_s, in_r, l1_s, l1_r, l2_s, l2_r),
        bb,
        cs,
        cr,
        ds,
        es,
        ru,
        rd,
    ) = grouped(refs, (6, 4, 20, 9, 15, 14, 12, chunks, chunks, chunks, turns, turns, turns, turns))
    place = lax.axis_index("spot")
    core = lax.axis_index("gene")
    z = place // PLANE
    q = place % PLANE
    col, row = q % 2, q // 2
    mates = ((1 - row) * 2 + 1 - col, row * 2 + 1 - col, (1 - row) * 2 + col)
    others = tuple((z + step) % lines for step in range(1, lines))
    up, down = (place + PLANE, core), (place - PLANE, core)
    sibling = (place, 1 - core)
    slides, slide_rows = logits_ref.shape[0], logits_ref.shape[1]
    rows = slides * slide_rows
    cb = expr_ref.shape[0]
    genes = expr_ref.shape[1]
    last = lines - 1

    def mate(p):
        return (z * PLANE + p, core)

    def send(src, dst, send_sem, recv_sem, device):
        copy = pltpu.make_async_remote_copy(
            src_ref=src, dst_ref=dst, send_sem=send_sem, recv_sem=recv_sem, device_id=device, device_id_type=MESH
        )
        copy.start()

    def arrived(dst, recv_sem):
        pltpu.make_async_copy(dst, dst, recv_sem).wait()

    sent = arrived

    def cols(k):
        return pl.ds(sum(forward_widths[:k]), forward_widths[k])

    def turn_cols(k):
        return pl.ds(sum(backward_widths[:k]), backward_widths[k])

    def block(index):
        return pl.ds(pl.multiple_of(index * cb, cb), cb)

    def share(index):
        return pl.ds(pl.multiple_of(index * rows, rows), rows)

    def half(index):
        return pl.ds(pl.multiple_of(index * slide_rows, slide_rows), slide_rows)

    small = ((prior_in, prior_ref), (count_in, count_ref), (cells_in, cells_ref))
    pltpu.make_async_copy(expr_ref, ex, loc.at[2 * slides]).start()
    for m in range(slides):
        pltpu.make_async_copy(logits_ref.at[m], lg.at[half(m)], loc.at[m]).start()
    for at, (src, dst) in enumerate(small):
        pltpu.make_async_copy(src, dst, loc.at[2 * slides + 1 + at]).start()
    for m in range(slides):
        pltpu.make_async_copy(spatial_ref.at[m], tg.at[half(m)], loc.at[slides + m]).start()

    barrier = pltpu.get_barrier_semaphore()
    for p in mates:
        pl.semaphore_signal(barrier, inc=1, device_id=mate(p), device_id_type=MESH)
    for o in others:
        pl.semaphore_signal(barrier, inc=1, device_id=(o * PLANE + q, core), device_id_type=MESH)
    pl.semaphore_signal(barrier, inc=1, device_id=sibling, device_id_type=MESH)
    pltpu.make_async_copy(expr_ref, ex, loc.at[2 * slides]).wait()
    for k in range(chunks):
        bb[k][block(z), :] = ex[:, cols(k)]
    for m in range(slides):
        pltpu.make_async_copy(logits_ref.at[m], lg.at[half(m)], loc.at[m]).wait()
    for p in range(PLANE):
        for line in range(lines):
            lq[p, :, pl.ds(line * cb, cb)] = lg[half(core), pl.ds((line * PLANE + p) * cb, cb)]
    pl.semaphore_wait(barrier, len(mates) + len(others) + 1)

    def own_up(k):
        here = bb[k].at[block(z)]
        send(here, here, ou_s.at[k], ou_r.at[k], up)

    def own_down(k):
        here = bb[k].at[block(z)]
        send(here, here, od_s.at[k], od_r.at[k], down)

    def low(at):
        return 2 * at < lines

    for at in range(lines):

        @pl.when(z == at)
        def _():
            for k in range(chunks):
                if at < last and (not low(at) or at == 0 or k < LEAD):
                    own_up(k)
                if at > 0 and (low(at) or at == last or k < LEAD):
                    own_down(k)

    for p in mates:
        send(lq.at[p], ab.at[q, half(core)], a_s, a_r.at[q], mate(p))

    def from_below(k, at):
        arrived(bb[k].at[pl.ds((at - 1) * cb, cb)], ou_r.at[k])
        if at > 1:
            arrived(bb[k].at[pl.ds(0, (at - 1) * cb)], fu_r.at[k])

    def from_above(k, at):
        arrived(bb[k].at[pl.ds((at + 1) * cb, cb)], od_r.at[k])
        if at < last - 1:
            arrived(bb[k].at[pl.ds((at + 2) * cb, (last - 1 - at) * cb)], fd_r.at[k])

    def upward(k, at):
        from_below(k, at)
        here = bb[k].at[pl.ds(0, at * cb)]
        send(here, here, fu_s.at[k], fu_r.at[k], up)

    def downward(k, at):
        from_above(k, at)
        here = bb[k].at[pl.ds((at + 1) * cb, (last - at) * cb)]
        send(here, here, fd_s.at[k], fd_r.at[k], down)

    def forward_far(k):
        for at in range(1, last):

            @pl.when(z == at)
            def _():
                (upward if low(at) else downward)(k, at)
                if k + LEAD < chunks:
                    (own_up if low(at) else own_down)(k + LEAD)

    def forward_near(k):
        for at in range(1, last):

            @pl.when(z == at)
            def _():
                (downward if low(at) else upward)(k, at)

    def gathered(k):
        @pl.when(z == 0)
        def _():
            from_above(k, 0)

        @pl.when(z == last)
        def _():
            from_below(k, last)

    for at, (src, dst) in enumerate(small):
        pltpu.make_async_copy(src, dst, loc.at[2 * slides + 1 + at]).wait()
    weights = prior_ref[...].astype(F32) / fixed_point

    @pl.loop(0, rows // STEP_ROWS)
    def _(step):
        at = pl.ds(pl.multiple_of(step * STEP_ROWS, STEP_ROWS), STEP_ROWS)
        value = lg[at, :]
        peak = jnp.max(value, axis=1, keepdims=True)
        raised = jnp.exp(value - peak)
        scale = 1.0 / jnp.sum(raised, axis=1, keepdims=True)
        probs = raised * scale
        mass_rows = jnp.sum(probs * weights, axis=1, keepdims=True)
        rowv[0, at, :] = jnp.broadcast_to(mass_rows, (STEP_ROWS, LANES))
        rowv[1, at, :] = jnp.broadcast_to(peak, (STEP_ROWS, LANES))
        rowv[2, at, :] = jnp.broadcast_to(scale, (STEP_ROWS, LANES))
        for p in range(PLANE):
            for line in range(lines):
                at_cells = (line * PLANE + p) * cb
                pq[p, at, pl.ds(line * cb, cb)] = probs[:, at_cells : at_cells + cb]

    wide = lax.broadcasted_iota(jnp.int32, (rows, LANES), 1)
    rs[q] = jnp.where(wide == 0, rowv[1], rowv[2]).T[0:8]
    for p in mates:
        send(rs.at[q], rs.at[q], r_s, r_r.at[q], mate(p))

    rid = lax.broadcasted_iota(jnp.int32, (rows, 1), 0)
    first = rid < slide_rows
    position = place * slide_rows + jnp.where(first, rid, rid - slide_rows)
    count = jnp.where(first, count_ref[0], count_ref[1])
    valid = (position < count).astype(F32)
    scale_count = count.astype(F32)
    square = (slide_rows, slide_rows)
    eye = lax.broadcasted_iota(jnp.int32, square, 0) == lax.broadcasted_iota(jnp.int32, square, 1)
    counted = jnp.concatenate(
        [
            jnp.sum(jnp.where(eye, cells_ref[m : m + 1, :].astype(F32), 0.0), axis=1, keepdims=True)
            for m in range(slides)
        ],
        axis=0,
    )
    mass = rowv[0, :, 0:1]
    kcell = valid * counted

    def by_slide(value):
        return [jnp.sum(value[m * slide_rows : (m + 1) * slide_rows], axis=0, keepdims=True) for m in range(slides)]

    mass_parts = by_slide(valid * mass)
    cell_parts = by_slide(kcell)
    lane = lax.broadcasted_iota(jnp.int32, (1, LANES), 1)
    scalars = jnp.zeros((1, LANES), F32)
    for at, value in enumerate(mass_parts + cell_parts):
        scalars = jnp.where(lane == at, value, scalars)
    for m in range(slides):
        pltpu.make_async_copy(spatial_ref.at[m], tg.at[half(m)], loc.at[slides + m]).wait()
    sacc[...] = jnp.zeros_like(sacc)
    s1[q, 3 * slides :, :] = jnp.zeros((8 - 3 * slides, genes), F32)
    s1[q, 3 * slides : 3 * slides + 1, 0:LANES] = scalars

    def share_logits():
        for p in (mates[1], mates[2], mates[0]):
            here = ab.at[p, half(core)]
            arrived(here, a_r.at[p])
            send(here, here, a2_s, a2_r.at[p], sibling)

    def take_probs():
        af[q] = pq[q]
        probs_3[share(q), :] = threefold(pq[q], 1, False)
        for p in (mates[1], mates[2], mates[0]):
            arrived(rs.at[p], r_r.at[p])
            arrived(ab.at[p, half(1 - core)], a2_r.at[p])
            by_row = rs[p].T
            probs = jnp.exp(ab[p] - by_row[:, 0:1]) * by_row[:, 1:2]
            af[p] = probs
            probs_3[share(p), :] = threefold(probs, 1, False)

    def transpose(part):
        for p in (2 * part, 2 * part + 1):
            high, low_part = halves(af[p].T)
            for at, value in enumerate((high, high, low_part)):
                turned_3[:, pl.ds(at * PLANE * rows + p * rows, rows)] = value

    def keep_expr(k, value):
        start = sum(forward_widths[:k])
        for turn in range(turns):
            origin, width = sum(backward_widths[:turn]), backward_widths[turn]
            lo, hi = max(start, origin), min(start + forward_widths[k], origin + width)
            if lo < hi:
                high, low_part = halves(value[:, lo - start : hi - start])
                for at, part in enumerate((high, low_part, high)):
                    expr_3[:, pl.ds(3 * origin + at * width + lo - origin, hi - lo)] = part

    def three_turn_cols(k):
        return pl.ds(3 * sum(backward_widths[:k]), 3 * backward_widths[k])

    def forward_product(k):
        value = bb[k][...]
        factor = threefold(value, 0, True)
        keep_expr(k, value)
        if k < chunks - 1:
            cs[k][...] = product(probs_3[...], factor, ((1,), (0,)))
            for p in mates:
                pass_pred(k, p)
        else:
            for side, served in ((1 - row, (mates[0], mates[2])), (row, (mates[1],))):
                pair = pl.ds(pl.multiple_of(2 * side * rows, 2 * rows), 2 * rows)
                cs[k][pair, :] = product(probs_3[pair, :], factor, ((1,), (0,)))
                for p in served:
                    pass_pred(k, p)

    def pass_pred(k, p):
        send(cs[k].at[share(p)], cr[k].at[q], c_s.at[k], c_r.at[k, q], mate(p))

    def finish_pred(k):
        total = cs[k][share(q), :]
        for p in mates:
            arrived(cr[k].at[p], c_r.at[k, p])
            total = total + cr[k][p]
        pr[:, cols(k)] = total
        truth = tg[:, cols(k)]
        for at, value in enumerate((total * truth, total * total, truth * truth)):
            sacc[at] += lane_groups(value)
        kept = valid * total
        stats = by_slide(kept * truth) + by_slide(kept * total) + by_slide(valid * truth * truth)
        s1[q, 0 : 3 * slides, cols(k)] = jnp.concatenate(stats, axis=0)

    early = sum(forward_widths[:EARLY])
    parts = (pl.ds(0, early), pl.ds(early, genes - early))

    def sum_plane(at):
        for p in mates:
            send(s1.at[q, :, parts[at]], s1.at[q, :, parts[at]], s1_s, s1_r.at[at, q], mate(p))

    def sum_line(at):
        for p in mates:
            arrived(s1.at[p, :, parts[at]], s1_r.at[at, p])
        s2[z, :, parts[at]] = (s1[0, :, parts[at]] + s1[1, :, parts[at]]) + (s1[2, :, parts[at]] + s1[3, :, parts[at]])
        for o in others:
            send(s2.at[z, :, parts[at]], s2.at[z, :, parts[at]], s2_s, s2_r.at[at, z], (o * PLANE + q, core))

    kept = {}

    def finish_genes(at):
        for o in others:
            arrived(s2.at[o, :, parts[at]], s2_r.at[at, o])
        total = s2[0, :, parts[at]]
        for line in range(1, lines):
            total = total + s2[line, :, parts[at]]
        gene_dot, gene_pred, gene_true = total[0:2], total[2:4], total[4:6]
        gene_inv = lax.rsqrt(gene_pred * gene_true + tiny)
        cos_gene = gene_dot * gene_inv
        gv[0:2, parts[at]] = gene_inv
        gv[2:4, parts[at]] = cos_gene * gene_true / (gene_pred * gene_true + tiny)
        kept["genes", at] = jnp.sum(jnp.sum(cos_gene, axis=1, keepdims=True), axis=0, keepdims=True)
        if at == 0:
            kept["mass"] = jnp.where(first, total[6:7, 0:1], total[6:7, 1:2])
            kept["cells"] = jnp.where(first, total[6:7, 2:3], total[6:7, 3:4])

    def sum_cores():
        sums = [jnp.sum(sacc[at], axis=1, keepdims=True) for at in range(3)]
        ss[core] = jnp.where(wide == 0, sums[0], jnp.where(wide == 1, sums[1], sums[2]))
        send(ss.at[core], ss.at[core], ss_s, ss_r, sibling)

    def finish_spots():
        arrived(ss.at[1 - core], ss_r)
        spot = ss[0] + ss[1]
        spot_dot, spot_pred, spot_true = spot[:, 0:1], spot[:, 1:2], spot[:, 2:3]
        spot_inv = lax.rsqrt(spot_pred * spot_true + tiny)
        cos_spot = spot_dot * spot_inv
        kept["inverse"], kept["cos"] = spot_inv, cos_spot
        kept["back"] = cos_spot * spot_true / (spot_pred * spot_true + tiny)
        sacc[0] = jnp.zeros_like(sacc[0])

    def send_grad(k):
        spot_inv, spot_back = kept["inverse"], kept["back"]
        pieces = []
        for m in range(slides):
            lo, hi = m * slide_rows, (m + 1) * slide_rows
            truth, guess = tg[lo:hi, turn_cols(k)], pr[lo:hi, turn_cols(k)]
            inverse, back = gv[m : m + 1, turn_cols(k)], gv[2 + m : 3 + m, turn_cols(k)]
            pieces.append(
                -valid[lo:hi]
                * (truth * (inverse + spot_inv[lo:hi]) - guess * back - guess * spot_back[lo:hi])
            )
        grad = jnp.concatenate(pieces, axis=0)
        here = ds[k].at[share(q)]
        here[...] = grad
        for p in mates:
            send(here, here, d_s.at[k], d_r.at[k, q], mate(p))
        sacc[0] += lane_groups(grad * pr[:, turn_cols(k)])

    def send_terms():
        mass_total, cell_total = kept["mass"], kept["cells"]
        portion = kcell / cell_total
        kl_rows = portion * (jnp.log(counted) - jnp.log(cell_total) - jnp.log(mass) + jnp.log(mass_total))
        dmass = scale_count * valid * (1.0 / mass_total - portion / mass)
        terms = jnp.sum(scale_count * kl_rows - valid * kept["cos"], axis=0, keepdims=True)
        l1[q] = jnp.broadcast_to(terms, (8, LANES))
        for p in mates:
            send(l1.at[q], l1.at[q], l1_s, l1_r.at[q], mate(p))
        inner = jnp.sum(sacc[0], axis=1, keepdims=True)
        inn[core] = jnp.where(wide == 0, inner, kept["genes", 0] + kept["genes", 1])
        send(inn.at[core], inn.at[core], in_s, in_r, sibling)
        rowv[1] = jnp.broadcast_to(dmass, (rows, LANES))

    middle = lines // 2

    def backward_product(k):
        for p in mates:
            arrived(ds[k].at[share(p)], d_r.at[k, p])
        value = ds[k][...]
        factor = threefold(value, 0, True)
        grad_3[:, three_turn_cols(k)] = threefold(value, 1, False)
        if not halved(k):
            es[k][...] = product(turned_3[...], factor, ((1,), (0,)))

        for turn in range(2):
            if halved(k):
                side = (1 - z // middle) if turn == 0 else z // middle
                pair = pl.ds(pl.multiple_of(side * middle * cb, middle * cb), middle * cb)
                es[k][pair, :] = product(turned_3[pair, :], factor, ((1,), (0,)))

            @pl.when(z == 0)
            def _():
                if halved(k):
                    pass_up(k, middle if turn == 0 else 1, middle if turn == 0 else middle - 1, turn)
                elif whole(k):
                    if turn == 0:
                        pass_up(k, 1, last, 0)
                elif turn == 0:
                    for line in range(last, 0, -1):
                        pass_up(k, line, 1, line)

            @pl.when(z == last)
            def _():
                if halved(k):
                    pass_down(k, 0 if turn == 0 else middle, middle if turn == 0 else middle - 1, turn)
                elif whole(k):
                    if turn == 0:
                        pass_down(k, 0, last, 0)
                elif turn == 0:
                    for line in range(last):
                        pass_down(k, line, 1, line)

    def halved(k):
        return k == 0

    def whole(k):
        return 0 < k < turns - SPLIT

    def pass_up(k, line, count, slot):
        here = pl.ds(line * cb, count * cb)
        send(es[k].at[here], ru[k].at[here], ru_s.at[k], ru_r.at[k, slot], up)

    def pass_down(k, line, count, slot):
        here = pl.ds(line * cb, count * cb)
        send(es[k].at[here], rd[k].at[here], rd_s.at[k], rd_r.at[k, slot], down)

    def take_up(k, line, count, slot):
        arrived(ru[k].at[pl.ds(line * cb, count * cb)], ru_r.at[k, slot])

    def take_down(k, line, count, slot):
        arrived(rd[k].at[pl.ds(line * cb, count * cb)], rd_r.at[k, slot])

    def add_up(k, line, count):
        here = pl.ds(line * cb, count * cb)
        es[k][here, :] += ru[k][here, :]

    def add_down(k, line, count):
        here = pl.ds(line * cb, count * cb)
        es[k][here, :] += rd[k][here, :]

    def rising(k, at):
        if halved(k) or whole(k):
            start = middle if halved(k) else at
            take_up(k, start, lines - start, 0)
            above = max(at + 1, start)
            add_up(k, above, lines - above)
            pass_up(k, above, lines - above, 0)
        else:
            for line in range(last, at, -1):
                take_up(k, line, 1, line)
                add_up(k, line, 1)
                pass_up(k, line, 1, line)

    def falling(k, at):
        if halved(k) or whole(k):
            end = middle if halved(k) else at + 1
            take_down(k, 0, end, 0)
            below = min(at, end)
            add_down(k, 0, below)
            pass_down(k, 0, below, 0)
        else:
            for line in range(at):
                take_down(k, line, 1, line)
                add_down(k, line, 1)
                pass_down(k, line, 1, line)

    def add_near(k):
        for at in range(1, last):

            @pl.when(z == at)
            def _():
                (rising if low(at) else falling)(k, at)

    def add_far(k):
        for at in range(1, last):

            @pl.when(z == at)
            def _():
                (falling if low(at) else rising)(k, at)

    def finish_expr(k):
        for at in range(lines):

            @pl.when(z == at)
            def _():
                own = pl.ds(at * cb, cb)
                total = es[k][own, :]
                if at > 0:
                    if halved(k) and at < middle:
                        take_up(k, at, 1, 1)
                    elif at == last and (halved(k) or whole(k)):
                        take_up(k, at, 1, 0)
                    elif not halved(k) and not whole(k):
                        take_up(k, at, 1, at)
                    total = total + ru[k][own, :]
                if at < last:
                    if halved(k) and at >= middle:
                        take_down(k, at, 1, 1)
                    elif at == 0 and (halved(k) or whole(k)):
                        take_down(k, at, 1, 0)
                    elif not halved(k) and not whole(k):
                        take_down(k, at, 1, at)
                    total = total + rd[k][own, :]
                ge[:, turn_cols(k)] = total

    def probs_gradient(k):
        at = three_turn_cols(k)
        part = product(grad_3[:, at], expr_3[:, at], ((1,), (1,)))
        if k == 0:
            fs[...] = part
        else:
            fs[...] += part

    def slide_of(p, m):
        return pl.ds(pl.multiple_of(p * rows + m * slide_rows, slide_rows), slide_rows)

    def sum_probs_cores():
        for p in mates + (q,):
            fx[p] = fs[slide_of(p, 1 - core), :]
            send(fx.at[p], fy.at[p], fx_s, fx_r.at[p], sibling)

    def return_probs():
        for p in mates:
            arrived(fy.at[p], fx_r.at[p])
            fz[p] = fs[slide_of(p, core), :] + fy[p]
            send(fz.at[p], fr.at[q], f_s, f_r.at[q], mate(p))
        arrived(fy.at[q], fx_r.at[q])
        fr[q] = fs[slide_of(q, core), :] + fy[q]

    def pass_terms():
        for p in mates:
            arrived(l1.at[p], l1_r.at[p])
        l2[z] = (l1[0] + l1[1]) + (l1[2] + l1[3])
        for o in others:
            send(l2.at[z], l2.at[z], l2_s, l2_r.at[z], (o * PLANE + q, core))

    def part_of(slide, m):
        start = slide * slide_rows + m * (slide_rows // 2)
        return pl.ds(pl.multiple_of(start, slide_rows // 2), slide_rows // 2)

    def finish_logits():
        arrived(inn.at[1 - core], in_r)
        rowv[2] = (inn[0] + inn[1]) + rowv[1] * rowv[0]
        for p in mates:
            arrived(fr.at[p], f_r.at[p])
        for m in range(2):

            @pl.loop(0, slide_rows // STEP_ROWS // 2)
            def _(step):
                row_at = (m * (slide_rows // STEP_ROWS // 2) + step) * STEP_ROWS
                at = pl.ds(pl.multiple_of(row_at, STEP_ROWS), STEP_ROWS)
                whole_at = pl.ds(pl.multiple_of(core * slide_rows + row_at, STEP_ROWS), STEP_ROWS)
                by_mass, total_inner = rowv[1, whole_at, 0:1], rowv[2, whole_at, 0:1]
                for p in range(PLANE):
                    for line in range(lines):
                        here, there = pl.ds(line * cb, cb), (line * PLANE + p) * cb
                        grad = fr[p, at, here] + by_mass * weights[:, there : there + cb]
                        glog[whole_at, pl.ds(there, cb)] = pq[p, whole_at, here] * (grad - total_inner)

            here = part_of(core, m)
            send(glog.at[here], glog.at[here], go_s, go_r.at[m], sibling)

    steps = {
        "far": forward_far,
        "near": forward_near,
        "share": share_logits,
        "take": take_probs,
        "whole": gathered,
        "product": forward_product,
        "sum": finish_pred,
        "turn": transpose,
        "plane": sum_plane,
        "line": sum_line,
        "genes": finish_genes,
        "cores": sum_cores,
        "spots": finish_spots,
        "grad": send_grad,
        "terms": send_terms,
        "backward": backward_product,
        "probs": probs_gradient,
        "exchange": sum_probs_cores,
        "return": return_probs,
        "loss": pass_terms,
        "logits": finish_logits,
        "add_near": add_near,
        "add_far": add_far,
        "expr": finish_expr,
    }
    for name, *where in STEPS:
        steps[name](*where)

    for o in others:
        arrived(l2.at[o], l2_r.at[o])
    loss = l2[0]
    for line in range(1, lines):
        loss = loss + l2[line]
    loss_ref[...] = loss[0:1, 0:1] - (inn[0, 0:1, 1:2] + inn[1, 0:1, 1:2])
    for m in range(2):
        arrived(glog.at[part_of(1 - core, m)], go_r.at[m])

    for k in range(chunks):

        @pl.when(z < last)
        def _():
            sent(bb[k].at[block(z)], ou_s.at[k])

        @pl.when(z > 0)
        def _():
            sent(bb[k].at[block(z)], od_s.at[k])

        for at in range(1, last):

            @pl.when(z == at)
            def _():
                sent(bb[k].at[pl.ds(0, at * cb)], fu_s.at[k])
                sent(bb[k].at[pl.ds((at + 1) * cb, (last - at) * cb)], fd_s.at[k])

    for k in range(turns):
        for at in range(lines):

            @pl.when(z == at)
            def _():
                if at < last:
                    sent(es[k].at[pl.ds((at + 1) * cb, (last - at) * cb)], ru_s.at[k])
                if at > 0:
                    sent(es[k].at[pl.ds(0, at * cb)], rd_s.at[k])

    three = pl.ds(0, len(mates))
    sent(ab.at[three, half(0)], a_s)
    sent(ab.at[three, half(0)], a2_s)
    sent(rs.at[three], r_s)
    for k in range(chunks):
        sent(cr[k].at[three], c_s.at[k])
    sent(s1.at[three], s1_s)
    sent(s2.at[pl.ds(0, last)], s2_s)
    sent(ss.at[0], ss_s)
    for k in range(turns):
        sent(ds[k].at[pl.ds(0, len(mates) * rows)], d_s.at[k])
    sent(inn.at[0], in_s)
    sent(l1.at[three], l1_s)
    sent(l2.at[pl.ds(0, last)], l2_s)
    sent(fr.at[three], f_s)
    sent(fx, fx_s)
    sent(glog.at[half(0)], go_s)


def lane_groups(value):
    parts = [value[:, at : at + LANES] for at in range(0, value.shape[1], LANES)]
    return functools.reduce(lambda a, b: a + b, parts)


def grouped(refs, sizes):
    at = 0
    for size in sizes:
        yield refs[at : at + size]
        at += size


def deliver(pred_in, loss_in, glog_in, gexp_in, pred_ref, loss_ref, glog_ref, gexp_ref, sems):
    slides, slide_rows = pred_ref.shape[0], pred_ref.shape[1]
    pairs = [(gexp_in, gexp_ref), (loss_in, loss_ref)]
    for m in range(slides):
        part = pl.ds(m * slide_rows, slide_rows)
        pairs += [(glog_in.at[part], glog_ref.at[m]), (pred_in.at[part], pred_ref.at[m])]
    copies = [pltpu.make_async_copy(src, dst, sems.at[at]) for at, (src, dst) in enumerate(pairs)]
    for copy in copies:
        copy.start()
    for copy in copies:
        copy.wait()


def plane_call(logits, expr, spatial, slide_spots, spot_cells, cell_prior, lines):
    slides, slide_rows, cells = logits.shape
    rows = slides * slide_rows
    cb, genes = expr.shape
    quarter = lines * cb
    spots = PLANE * rows
    chunks, turns = len(FORWARD), len(BACKWARD)
    dma = pltpu.SemaphoreType.DMA
    vmem = pltpu.VMEM
    anywhere = pl.BlockSpec(memory_space=pl.ANY)
    in_vmem = pl.BlockSpec(memory_space=pltpu.VMEM)
    scratch = [
        pltpu.SMEM((slides,), jnp.int32),
        vmem((slides, slide_rows), jnp.int32),
        vmem((1, cells), jnp.int32),
        vmem((rows, cells), F32),
        vmem((PLANE, slide_rows, quarter), F32),
        vmem((rows, genes), F32),
        vmem((cb, genes), F32),
        vmem((PLANE, rows, quarter), F32),
        vmem((PLANE, rows, quarter), F32),
        vmem((PLANE, rows, quarter), F32),
        vmem((spots, 3 * quarter), BF16),
        vmem((quarter, 3 * spots), BF16),
        vmem((quarter, 3 * genes), BF16),
        vmem((3, rows, LANES), F32),
        vmem((PLANE, 8, genes), F32),
        vmem((lines, 8, genes), F32),
        vmem((8, genes), F32),
        vmem((2, rows, LANES), F32),
        vmem((3, rows, LANES), F32),
        vmem((PLANE, 8, rows), F32),
        vmem((spots, 3 * genes), BF16),
        vmem((spots, quarter), F32),
        vmem((PLANE, slide_rows, quarter), F32),
        vmem((PLANE, slide_rows, quarter), F32),
        vmem((PLANE, slide_rows, quarter), F32),
        vmem((PLANE, slide_rows, quarter), F32),
        vmem((2, rows, LANES), F32),
        vmem((PLANE, 8, LANES), F32),
        vmem((lines, 8, LANES), F32),
        dma((2 * slides + 4,)),
        dma((chunks,)),
        dma((chunks,)),
        dma((chunks,)),
        dma((chunks,)),
        dma((chunks,)),
        dma((chunks,)),
        dma((chunks,)),
        dma((chunks,)),
        dma,
        dma((PLANE,)),
        dma,
        dma((PLANE,)),
        dma,
        dma((PLANE,)),
        dma((chunks,)),
        dma((chunks, PLANE)),
        dma,
        dma((2, PLANE)),
        dma,
        dma((2, lines)),
        dma,
        dma,
        dma((turns,)),
        dma((turns, PLANE)),
        dma((turns,)),
        dma((turns, lines)),
        dma((turns,)),
        dma((turns, lines)),
        dma,
        dma((PLANE,)),
        dma,
        dma((PLANE,)),
        dma,
        dma((2,)),
        dma,
        dma,
        dma,
        dma((PLANE,)),
        dma,
        dma((lines,)),
    ]
    for shape, widths in (
        ((quarter,), FORWARD),
        ((spots,), FORWARD),
        ((PLANE, rows), FORWARD),
        ((spots,), BACKWARD),
        ((quarter,), BACKWARD),
        ((quarter,), BACKWARD),
        ((quarter,), BACKWARD),
    ):
        scratch += [vmem(shape + (width,), F32) for width in widths]
    in_hbm = functools.partial(pltpu.with_memory_space_constraint, memory_space=pltpu.HBM)
    in_place = functools.partial(pltpu.with_memory_space_constraint, memory_space=pltpu.VMEM)
    results = pl.pallas_call(
        functools.partial(plane_kernel, lines, FORWARD, BACKWARD),
        out_shape=(
            vmem((rows, genes), F32),
            vmem((1, 1), F32),
            vmem((rows, cells), F32),
            vmem((cb, genes), F32),
        ),
        in_specs=[anywhere] * 6,
        out_specs=(in_vmem,) * 4,
        scratch_shapes=scratch,
        compiler_params=pltpu.CompilerParams(
            collective_id=0, has_side_effects=True, vmem_limit_bytes=48 * 1024 * 1024
        ),
    )(*map(in_hbm, (logits, expr, spatial, slide_spots, spot_cells, cell_prior.reshape(1, cells))))
    pred, loss, grad_logits, grad_expr = pl.pallas_call(
        deliver,
        out_shape=(
            jax.ShapeDtypeStruct((slides, slide_rows, genes), F32),
            jax.ShapeDtypeStruct((1, 1), F32),
            jax.ShapeDtypeStruct((slides, slide_rows, cells), F32),
            jax.ShapeDtypeStruct((cb, genes), F32),
        ),
        in_specs=[anywhere] * 4,
        out_specs=(anywhere,) * 4,
        scratch_shapes=[dma((2 * slides + 2,))],
        compiler_params=pltpu.CompilerParams(vmem_limit_bytes=4 * 1024 * 1024),
    )(*map(in_place, results))
    return pred, loss.reshape(()), grad_logits, grad_expr


def general_plan(logits, expr, spatial, slide_spots, spot_cells, cell_prior):
    place = lax.axis_index("spot")
    side = lax.axis_index("gene")
    rows_all = logits.shape[1]
    cell_rows = expr.shape[0]
    weights = cell_prior.astype(jnp.float32) / fixed_point
    gene_share = (place == 0).astype(jnp.float32)
    row_share = (side == 0).astype(jnp.float32)
    own_weights = lax.dynamic_slice_in_dim(weights, place * cell_rows, cell_rows, 0)
    expr_acc = jnp.zeros((cell_rows, expr.shape[1]), jnp.float32)
    loss_local = jnp.zeros((), jnp.float32)
    pred_list = []
    grad_list = []
    for slide in range(logits.shape[0]):
        logit_rows = logits[slide]
        counted = spot_cells[slide].astype(jnp.float32)
        target = spatial[slide]
        positions = place * rows_all + jnp.arange(rows_all, dtype=jnp.int32)
        valid = (positions < slide_spots[slide]).astype(jnp.float32)
        peak = jnp.max(logit_rows, axis=1, keepdims=True)
        raised = jnp.exp(logit_rows - peak)
        probs = raised / jnp.sum(raised, axis=1, keepdims=True)
        mass = jnp.dot(probs, weights, precision=lax.Precision.HIGHEST)
        blocks = lax.all_to_all(probs, "spot", split_axis=1, concat_axis=0, tiled=True)
        pred = lax.psum_scatter(
            jnp.dot(blocks, expr, precision=lax.Precision.HIGHEST),
            "spot",
            scatter_dimension=0,
            tiled=True,
        )
        gene_dot = jnp.sum(valid[:, None] * pred * target, axis=0)
        gene_pred = jnp.sum(valid[:, None] * pred * pred, axis=0)
        gene_true = jnp.sum(valid[:, None] * target * target, axis=0)
        mass_part = jnp.sum(valid * mass)
        kcell = valid * counted
        cell_part = jnp.sum(kcell)
        spot_dot = jnp.sum(pred * target, axis=1)
        spot_pred = jnp.sum(pred * pred, axis=1)
        spot_true = jnp.sum(target * target, axis=1)
        gene_dot, gene_pred, gene_true, mass_total, cell_total = lax.psum(
            (gene_dot, gene_pred, gene_true, mass_part, cell_part), "spot"
        )
        spot_dot, spot_pred, spot_true = lax.psum((spot_dot, spot_pred, spot_true), "gene")
        gene_inv = lax.rsqrt(gene_pred * gene_true + tiny)
        cos_gene = gene_dot * gene_inv
        spot_inv = lax.rsqrt(spot_pred * spot_true + tiny)
        cos_spot = spot_dot * spot_inv
        share = kcell / cell_total
        scale_count = slide_spots[slide].astype(jnp.float32)
        kl_part = jnp.sum(
            share * (jnp.log(counted) - jnp.log(cell_total) - jnp.log(mass) + jnp.log(mass_total))
        )
        loss_local = loss_local - gene_share * jnp.sum(cos_gene)
        loss_local = loss_local + row_share * (scale_count * kl_part - jnp.sum(valid * cos_spot))
        gene_back = cos_gene * gene_true / (gene_pred * gene_true + tiny)
        spot_back = cos_spot * spot_true / (spot_pred * spot_true + tiny)
        dpred = -valid[:, None] * (
            target * (gene_inv[None, :] + spot_inv[:, None])
            - pred * gene_back[None, :]
            - pred * spot_back[:, None]
        )
        dmass = scale_count * valid * (1.0 / mass_total - share / mass)
        pred_list.append(pred)
        grads_full, mass_full = (
            lax.all_gather(dpred, "spot", axis=0, tiled=True),
            lax.all_gather(dmass, "spot", axis=0, tiled=True),
        )
        dprob_cells = jnp.dot(grads_full, expr.T, precision=lax.Precision.HIGHEST)
        dprob_cells = lax.psum(dprob_cells, "gene")
        expr_acc = expr_acc + lax.dot_general(
            blocks, grads_full, (((0,), (0,)), ((), ())), precision=lax.Precision.HIGHEST
        )
        dprob_cells = dprob_cells + mass_full[:, None] * own_weights[None, :]
        dprob_rows = lax.all_to_all(dprob_cells, "spot", split_axis=0, concat_axis=1, tiled=True)
        inner = jnp.sum(probs * dprob_rows, axis=1, keepdims=True)
        dlogit = probs * (dprob_rows - inner)
        grad_list.append(dlogit)
    loss = lax.psum(loss_local, ("spot", "gene"))
    return (jnp.stack(pred_list), loss, jnp.stack(grad_list), expr_acc)


def solution(mesh):
    places = mesh.shape["spot"]

    def on_device(logits, expr, spatial, slide_spots, spot_cells, cell_prior):
        if places == PLANE * PLANE and mesh.shape["gene"] == 2 and expr.shape[1] == sum(FORWARD):
            return plane_call(
                logits, expr, spatial, slide_spots, spot_cells, cell_prior, places // PLANE
            )
        return general_plan(logits, expr, spatial, slide_spots, spot_cells, cell_prior)

    in_specs = (
        P(None, "spot", None),
        P("spot", "gene"),
        P(None, "spot", "gene"),
        P(),
        P(None, "spot"),
        P(),
    )
    out_specs = (P(None, "spot", "gene"), P(), P(None, "spot", None), P("spot", "gene"))
    return jax.shard_map(
        on_device, mesh=mesh, in_specs=in_specs, out_specs=out_specs, check_vma=False
    )
```

```python
import functools

import jax
import jax.numpy as jnp
from jax import lax
from jax.experimental import pallas as pl
from jax.experimental.pallas import tpu as pltpu
from jax.sharding import PartitionSpec as P

tiny = 1e-06
fixed_point = 16384.0
F32 = jnp.float32
BF16 = jnp.bfloat16
MESH = pl.DeviceIdType.MESH

PLANE = 4
LANES = 128
STEP_ROWS = 16
FORWARD = (128, 256, 256, 256, 128)
BACKWARD = (128, 128, 256, 256, 256)
SPLIT = 2
LEAD = 2
NEAR_LEAD = 3
EARLY = 4
STEPS = (
    ("far", 0),
    ("far", 1),
    ("near", 0),
    ("share",),
    ("whole", 0),
    ("far", 2),
    ("far", 3),
    ("take",),
    ("near", 1),
    ("turn", 0),
    ("product", 0),
    ("near", 2),
    ("sum", 0),
    ("whole", 1),
    ("product", 1),
    ("near", 3),
    ("turn", 1),
    ("whole", 2),
    ("product", 2),
    ("whole", 3),
    ("product", 3),
    ("whole", 4),
    ("far", 4),
    ("sum", 1),
    ("near", 4),
    ("sum", 2),
    ("product", 4),
    ("sum", 3),
    ("plane", 0),
    ("sum", 4),
    ("plane", 1),
    ("cores",),
    ("line", 0),
    ("line", 1),
    ("spots",),
    ("genes", 0),
    ("grad", 0),
    ("grad", 1),
    ("grad", 2),
    ("backward", 0),
    ("backward", 1),
    ("grad", 3),
    ("probs", 0),
    ("add_near", 0),
    ("backward", 2),
    ("genes", 1),
    ("probs", 1),
    ("add_far", 0),
    ("probs", 2),
    ("grad", 4),
    ("terms",),
    ("add_near", 1),
    ("backward", 3),
    ("probs", 3),
    ("add_near", 2),
    ("add_far", 1),
    ("backward", 4),
    ("expr", 0),
    ("probs", 4),
    ("exchange",),
    ("add_near", 3),
    ("add_far", 2),
    ("return",),
    ("loss",),
    ("expr", 1),
    ("expr", 2),
    ("add_far", 3),
    ("add_near", 4),
    ("logits",),
    ("add_far", 4),
    ("expr", 3),
    ("expr", 4),
)


def halves(value):
    high = value.astype(BF16)
    return high, (value - high.astype(F32)).astype(BF16)


def threefold(value, axis, mixed):
    high, low = halves(value)
    return jnp.concatenate([high, low, high] if mixed else [high, high, low], axis=axis)


def product(a, b, contract):
    return lax.dot_general(a, b, (contract, ((), ())), preferred_element_type=F32)


def plane_kernel(lines, forward_widths, backward_widths, *refs):
    chunks, turns = len(forward_widths), len(backward_widths)
    (
        (logits_ref, expr_ref, spatial_ref, count_in, cells_in, prior_in),
        (pr, loss_ref, glog, ge),
        (count_ref, cells_ref, prior_ref, lg, lq, tg, ex, pq, ab, af, probs_3, turned_3, expr_3, sacc, s1, s2, gv, ss, rowv, rs),
        (grad_3, fs, fx, fy, fz, fr, inn, l1, l2),
        (loc, ou_s, ou_r, od_s, od_r, fu_s, fu_r, fd_s, fd_r, a_s, a_r, a2_s, a2_r, r_s, r_r),
        (c_s, c_r, s1_s, s1_r, s2_s, s2_r, ss_s, ss_r, d_s, d_r, ru_s, ru_r, rd_s, rd_r),
        (f_s, f_r, fx_s, fx_r, go_s, go_r, in_s, in_r, l1_s, l1_r, l2_s, l2_r),
        bb,
        cs,
        cr,
        ds,
        es,
        ru,
        rd,
    ) = grouped(refs, (6, 4, 20, 9, 15, 14, 12, chunks, chunks, chunks, turns, turns, turns, turns))
    place = lax.axis_index("spot")
    core = lax.axis_index("gene")
    z = place // PLANE
    q = place % PLANE
    col, row = q % 2, q // 2
    mates = ((1 - row) * 2 + 1 - col, row * 2 + 1 - col, (1 - row) * 2 + col)
    others = tuple((z + step) % lines for step in range(1, lines))
    up, down = (place + PLANE, core), (place - PLANE, core)
    sibling = (place, 1 - core)
    slides, slide_rows = logits_ref.shape[0], logits_ref.shape[1]
    rows = slides * slide_rows
    cb = expr_ref.shape[0]
    genes = expr_ref.shape[1]
    last = lines - 1

    def mate(p):
        return (z * PLANE + p, core)

    def send(src, dst, send_sem, recv_sem, device):
        copy = pltpu.make_async_remote_copy(
            src_ref=src, dst_ref=dst, send_sem=send_sem, recv_sem=recv_sem, device_id=device, device_id_type=MESH
        )
        copy.start()

    def arrived(dst, recv_sem):
        pltpu.make_async_copy(dst, dst, recv_sem).wait()

    sent = arrived

    def cols(k):
        return pl.ds(sum(forward_widths[:k]), forward_widths[k])

    def turn_cols(k):
        return pl.ds(sum(backward_widths[:k]), backward_widths[k])

    def block(index):
        return pl.ds(pl.multiple_of(index * cb, cb), cb)

    def share(index):
        return pl.ds(pl.multiple_of(index * rows, rows), rows)

    def half(index):
        return pl.ds(pl.multiple_of(index * slide_rows, slide_rows), slide_rows)

    small = ((prior_in, prior_ref), (count_in, count_ref), (cells_in, cells_ref))
    pltpu.make_async_copy(expr_ref, ex, loc.at[2 * slides]).start()
    for m in range(slides):
        pltpu.make_async_copy(logits_ref.at[m], lg.at[half(m)], loc.at[m]).start()
    for at, (src, dst) in enumerate(small):
        pltpu.make_async_copy(src, dst, loc.at[2 * slides + 1 + at]).start()
    for m in range(slides):
        pltpu.make_async_copy(spatial_ref.at[m], tg.at[half(m)], loc.at[slides + m]).start()

    barrier = pltpu.get_barrier_semaphore()
    for p in mates:
        pl.semaphore_signal(barrier, inc=1, device_id=mate(p), device_id_type=MESH)
    for o in others:
        pl.semaphore_signal(barrier, inc=1, device_id=(o * PLANE + q, core), device_id_type=MESH)
    pl.semaphore_signal(barrier, inc=1, device_id=sibling, device_id_type=MESH)
    pltpu.make_async_copy(expr_ref, ex, loc.at[2 * slides]).wait()
    for k in range(chunks):
        bb[k][block(z), :] = ex[:, cols(k)]
    for m in range(slides):
        pltpu.make_async_copy(logits_ref.at[m], lg.at[half(m)], loc.at[m]).wait()
    for p in range(PLANE):
        for line in range(lines):
            lq[p, :, pl.ds(line * cb, cb)] = lg[half(core), pl.ds((line * PLANE + p) * cb, cb)]
    pl.semaphore_wait(barrier, len(mates) + len(others) + 1)

    def own_up(k):
        here = bb[k].at[block(z)]
        send(here, here, ou_s.at[k], ou_r.at[k], up)

    def own_down(k):
        here = bb[k].at[block(z)]
        send(here, here, od_s.at[k], od_r.at[k], down)

    def low(at):
        return 2 * at < lines

    for at in range(lines):

        @pl.when(z == at)
        def _():
            for k in range(chunks):
                if at < last and (at == 0 or k < (LEAD if low(at) else NEAR_LEAD)):
                    own_up(k)
                if at > 0 and (at == last or k < (NEAR_LEAD if low(at) else LEAD)):
                    own_down(k)

    for p in mates:
        send(lq.at[p], ab.at[q, half(core)], a_s, a_r.at[q], mate(p))

    def from_below(k, at):
        arrived(bb[k].at[pl.ds((at - 1) * cb, cb)], ou_r.at[k])
        if at > 1:
            arrived(bb[k].at[pl.ds(0, (at - 1) * cb)], fu_r.at[k])

    def from_above(k, at):
        arrived(bb[k].at[pl.ds((at + 1) * cb, cb)], od_r.at[k])
        if at < last - 1:
            arrived(bb[k].at[pl.ds((at + 2) * cb, (last - 1 - at) * cb)], fd_r.at[k])

    def upward(k, at):
        from_below(k, at)
        here = bb[k].at[pl.ds(0, at * cb)]
        send(here, here, fu_s.at[k], fu_r.at[k], up)

    def downward(k, at):
        from_above(k, at)
        here = bb[k].at[pl.ds((at + 1) * cb, (last - at) * cb)]
        send(here, here, fd_s.at[k], fd_r.at[k], down)

    def forward_far(k):
        for at in range(1, last):

            @pl.when(z == at)
            def _():
                (upward if low(at) else downward)(k, at)
                if k + LEAD < chunks:
                    (own_up if low(at) else own_down)(k + LEAD)

    def forward_near(k):
        for at in range(1, last):

            @pl.when(z == at)
            def _():
                (downward if low(at) else upward)(k, at)
                if k + NEAR_LEAD < chunks:
                    (own_down if low(at) else own_up)(k + NEAR_LEAD)

    def gathered(k):
        @pl.when(z == 0)
        def _():
            from_above(k, 0)

        @pl.when(z == last)
        def _():
            from_below(k, last)

    for at, (src, dst) in enumerate(small):
        pltpu.make_async_copy(src, dst, loc.at[2 * slides + 1 + at]).wait()
    weights = prior_ref[...].astype(F32) / fixed_point

    @pl.loop(0, rows // STEP_ROWS)
    def _(step):
        at = pl.ds(pl.multiple_of(step * STEP_ROWS, STEP_ROWS), STEP_ROWS)
        value = lg[at, :]
        peak = jnp.max(value, axis=1, keepdims=True)
        raised = jnp.exp(value - peak)
        scale = 1.0 / jnp.sum(raised, axis=1, keepdims=True)
        probs = raised * scale
        mass_rows = jnp.sum(probs * weights, axis=1, keepdims=True)
        rowv[0, at, :] = jnp.broadcast_to(mass_rows, (STEP_ROWS, LANES))
        rowv[1, at, :] = jnp.broadcast_to(peak, (STEP_ROWS, LANES))
        rowv[2, at, :] = jnp.broadcast_to(scale, (STEP_ROWS, LANES))
        for p in range(PLANE):
            for line in range(lines):
                at_cells = (line * PLANE + p) * cb
                pq[p, at, pl.ds(line * cb, cb)] = probs[:, at_cells : at_cells + cb]

    wide = lax.broadcasted_iota(jnp.int32, (rows, LANES), 1)
    rs[q] = jnp.where(wide == 0, rowv[1], rowv[2]).T[0:8]
    for p in mates:
        send(rs.at[q], rs.at[q], r_s, r_r.at[q], mate(p))

    rid = lax.broadcasted_iota(jnp.int32, (rows, 1), 0)
    first = rid < slide_rows
    position = place * slide_rows + jnp.where(first, rid, rid - slide_rows)
    count = jnp.where(first, count_ref[0], count_ref[1])
    valid = (position < count).astype(F32)
    scale_count = count.astype(F32)
    square = (slide_rows, slide_rows)
    eye = lax.broadcasted_iota(jnp.int32, square, 0) == lax.broadcasted_iota(jnp.int32, square, 1)
    counted = jnp.concatenate(
        [
            jnp.sum(jnp.where(eye, cells_ref[m : m + 1, :].astype(F32), 0.0), axis=1, keepdims=True)
            for m in range(slides)
        ],
        axis=0,
    )
    mass = rowv[0, :, 0:1]
    kcell = valid * counted

    def by_slide(value):
        return [jnp.sum(value[m * slide_rows : (m + 1) * slide_rows], axis=0, keepdims=True) for m in range(slides)]

    mass_parts = by_slide(valid * mass)
    cell_parts = by_slide(kcell)
    lane = lax.broadcasted_iota(jnp.int32, (1, LANES), 1)
    scalars = jnp.zeros((1, LANES), F32)
    for at, value in enumerate(mass_parts + cell_parts):
        scalars = jnp.where(lane == at, value, scalars)
    for m in range(slides):
        pltpu.make_async_copy(spatial_ref.at[m], tg.at[half(m)], loc.at[slides + m]).wait()
    sacc[...] = jnp.zeros_like(sacc)
    s1[q, 3 * slides :, :] = jnp.zeros((8 - 3 * slides, genes), F32)
    s1[q, 3 * slides : 3 * slides + 1, 0:LANES] = scalars

    def share_logits():
        for p in (mates[1], mates[2], mates[0]):
            here = ab.at[p, half(core)]
            arrived(here, a_r.at[p])
            send(here, here, a2_s, a2_r.at[p], sibling)

    def take_probs():
        af[q] = pq[q]
        probs_3[share(q), :] = threefold(pq[q], 1, False)
        for p in (mates[1], mates[2], mates[0]):
            arrived(rs.at[p], r_r.at[p])
            arrived(ab.at[p, half(1 - core)], a2_r.at[p])
            by_row = rs[p].T
            probs = jnp.exp(ab[p] - by_row[:, 0:1]) * by_row[:, 1:2]
            af[p] = probs
            probs_3[share(p), :] = threefold(probs, 1, False)

    def transpose(part):
        for p in (2 * part, 2 * part + 1):
            high, low_part = halves(af[p].T)
            for at, value in enumerate((high, high, low_part)):
                turned_3[:, pl.ds(at * PLANE * rows + p * rows, rows)] = value

    def keep_expr(k, value):
        start = sum(forward_widths[:k])
        for turn in range(turns):
            origin, width = sum(backward_widths[:turn]), backward_widths[turn]
            lo, hi = max(start, origin), min(start + forward_widths[k], origin + width)
            if lo < hi:
                high, low_part = halves(value[:, lo - start : hi - start])
                for at, part in enumerate((high, low_part, high)):
                    expr_3[:, pl.ds(3 * origin + at * width + lo - origin, hi - lo)] = part

    def three_turn_cols(k):
        return pl.ds(3 * sum(backward_widths[:k]), 3 * backward_widths[k])

    def forward_product(k):
        value = bb[k][...]
        factor = threefold(value, 0, True)
        keep_expr(k, value)
        if k < chunks - 1:
            cs[k][...] = product(probs_3[...], factor, ((1,), (0,)))
            for p in mates:
                pass_pred(k, p)
        else:
            for side, served in ((1 - row, (mates[0], mates[2])), (row, (mates[1],))):
                pair = pl.ds(pl.multiple_of(2 * side * rows, 2 * rows), 2 * rows)
                cs[k][pair, :] = product(probs_3[pair, :], factor, ((1,), (0,)))
                for p in served:
                    pass_pred(k, p)

    def pass_pred(k, p):
        send(cs[k].at[share(p)], cr[k].at[q], c_s.at[k], c_r.at[k, q], mate(p))

    def finish_pred(k):
        total = cs[k][share(q), :]
        for p in mates:
            arrived(cr[k].at[p], c_r.at[k, p])
            total = total + cr[k][p]
        pr[:, cols(k)] = total
        truth = tg[:, cols(k)]
        for at, value in enumerate((total * truth, total * total, truth * truth)):
            sacc[at] += lane_groups(value)
        kept = valid * total
        stats = by_slide(kept * truth) + by_slide(kept * total) + by_slide(valid * truth * truth)
        s1[q, 0 : 3 * slides, cols(k)] = jnp.concatenate(stats, axis=0)

    early = sum(forward_widths[:EARLY])
    parts = (pl.ds(0, early), pl.ds(early, genes - early))

    def sum_plane(at):
        for p in mates:
            send(s1.at[q, :, parts[at]], s1.at[q, :, parts[at]], s1_s, s1_r.at[at, q], mate(p))

    def sum_line(at):
        for p in mates:
            arrived(s1.at[p, :, parts[at]], s1_r.at[at, p])
        s2[z, :, parts[at]] = (s1[0, :, parts[at]] + s1[1, :, parts[at]]) + (s1[2, :, parts[at]] + s1[3, :, parts[at]])
        for o in others:
            send(s2.at[z, :, parts[at]], s2.at[z, :, parts[at]], s2_s, s2_r.at[at, z], (o * PLANE + q, core))

    kept = {}

    def finish_genes(at):
        for o in others:
            arrived(s2.at[o, :, parts[at]], s2_r.at[at, o])
        total = s2[0, :, parts[at]]
        for line in range(1, lines):
            total = total + s2[line, :, parts[at]]
        gene_dot, gene_pred, gene_true = total[0:2], total[2:4], total[4:6]
        gene_inv = lax.rsqrt(gene_pred * gene_true + tiny)
        cos_gene = gene_dot * gene_inv
        gv[0:2, parts[at]] = gene_inv
        gv[2:4, parts[at]] = cos_gene * gene_true / (gene_pred * gene_true + tiny)
        kept["genes", at] = jnp.sum(jnp.sum(cos_gene, axis=1, keepdims=True), axis=0, keepdims=True)
        if at == 0:
            kept["mass"] = jnp.where(first, total[6:7, 0:1], total[6:7, 1:2])
            kept["cells"] = jnp.where(first, total[6:7, 2:3], total[6:7, 3:4])

    def sum_cores():
        sums = [jnp.sum(sacc[at], axis=1, keepdims=True) for at in range(3)]
        ss[core] = jnp.where(wide == 0, sums[0], jnp.where(wide == 1, sums[1], sums[2]))
        send(ss.at[core], ss.at[core], ss_s, ss_r, sibling)

    def finish_spots():
        arrived(ss.at[1 - core], ss_r)
        spot = ss[0] + ss[1]
        spot_dot, spot_pred, spot_true = spot[:, 0:1], spot[:, 1:2], spot[:, 2:3]
        spot_inv = lax.rsqrt(spot_pred * spot_true + tiny)
        cos_spot = spot_dot * spot_inv
        kept["inverse"], kept["cos"] = spot_inv, cos_spot
        kept["back"] = cos_spot * spot_true / (spot_pred * spot_true + tiny)
        sacc[0] = jnp.zeros_like(sacc[0])

    def send_grad(k):
        spot_inv, spot_back = kept["inverse"], kept["back"]
        pieces = []
        for m in range(slides):
            lo, hi = m * slide_rows, (m + 1) * slide_rows
            truth, guess = tg[lo:hi, turn_cols(k)], pr[lo:hi, turn_cols(k)]
            inverse, back = gv[m : m + 1, turn_cols(k)], gv[2 + m : 3 + m, turn_cols(k)]
            pieces.append(
                -valid[lo:hi]
                * (truth * (inverse + spot_inv[lo:hi]) - guess * back - guess * spot_back[lo:hi])
            )
        grad = jnp.concatenate(pieces, axis=0)
        here = ds[k].at[share(q)]
        here[...] = grad
        for p in mates:
            send(here, here, d_s.at[k], d_r.at[k, q], mate(p))
        sacc[0] += lane_groups(grad * pr[:, turn_cols(k)])

    def send_terms():
        mass_total, cell_total = kept["mass"], kept["cells"]
        portion = kcell / cell_total
        kl_rows = portion * (jnp.log(counted) - jnp.log(cell_total) - jnp.log(mass) + jnp.log(mass_total))
        dmass = scale_count * valid * (1.0 / mass_total - portion / mass)
        terms = jnp.sum(scale_count * kl_rows - valid * kept["cos"], axis=0, keepdims=True)
        l1[q] = jnp.broadcast_to(terms, (8, LANES))
        for p in mates:
            send(l1.at[q], l1.at[q], l1_s, l1_r.at[q], mate(p))
        inner = jnp.sum(sacc[0], axis=1, keepdims=True)
        inn[core] = jnp.where(wide == 0, inner, kept["genes", 0] + kept["genes", 1])
        send(inn.at[core], inn.at[core], in_s, in_r, sibling)
        rowv[1] = jnp.broadcast_to(dmass, (rows, LANES))

    middle = lines // 2

    def backward_product(k):
        for p in mates:
            arrived(ds[k].at[share(p)], d_r.at[k, p])
        value = ds[k][...]
        factor = threefold(value, 0, True)
        grad_3[:, three_turn_cols(k)] = threefold(value, 1, False)
        if not halved(k):
            es[k][...] = product(turned_3[...], factor, ((1,), (0,)))

        for turn in range(2):
            if halved(k):
                side = (1 - z // middle) if turn == 0 else z // middle
                pair = pl.ds(pl.multiple_of(side * middle * cb, middle * cb), middle * cb)
                es[k][pair, :] = product(turned_3[pair, :], factor, ((1,), (0,)))

            @pl.when(z == 0)
            def _():
                if halved(k):
                    pass_up(k, middle if turn == 0 else 1, middle if turn == 0 else middle - 1, turn)
                elif whole(k):
                    if turn == 0:
                        pass_up(k, 1, last, 0)
                elif turn == 0:
                    for line in range(last, 0, -1):
                        pass_up(k, line, 1, line)

            @pl.when(z == last)
            def _():
                if halved(k):
                    pass_down(k, 0 if turn == 0 else middle, middle if turn == 0 else middle - 1, turn)
                elif whole(k):
                    if turn == 0:
                        pass_down(k, 0, last, 0)
                elif turn == 0:
                    for line in range(last):
                        pass_down(k, line, 1, line)

    def halved(k):
        return k == 0

    def whole(k):
        return 0 < k < turns - SPLIT

    def pass_up(k, line, count, slot):
        here = pl.ds(line * cb, count * cb)
        send(es[k].at[here], ru[k].at[here], ru_s.at[k], ru_r.at[k, slot], up)

    def pass_down(k, line, count, slot):
        here = pl.ds(line * cb, count * cb)
        send(es[k].at[here], rd[k].at[here], rd_s.at[k], rd_r.at[k, slot], down)

    def take_up(k, line, count, slot):
        arrived(ru[k].at[pl.ds(line * cb, count * cb)], ru_r.at[k, slot])

    def take_down(k, line, count, slot):
        arrived(rd[k].at[pl.ds(line * cb, count * cb)], rd_r.at[k, slot])

    def add_up(k, line, count):
        here = pl.ds(line * cb, count * cb)
        es[k][here, :] += ru[k][here, :]

    def add_down(k, line, count):
        here = pl.ds(line * cb, count * cb)
        es[k][here, :] += rd[k][here, :]

    def rising(k, at):
        if halved(k) or whole(k):
            start = middle if halved(k) else at
            take_up(k, start, lines - start, 0)
            above = max(at + 1, start)
            add_up(k, above, lines - above)
            pass_up(k, above, lines - above, 0)
        else:
            for line in range(last, at, -1):
                take_up(k, line, 1, line)
                add_up(k, line, 1)
                pass_up(k, line, 1, line)

    def falling(k, at):
        if halved(k) or whole(k):
            end = middle if halved(k) else at + 1
            take_down(k, 0, end, 0)
            below = min(at, end)
            add_down(k, 0, below)
            pass_down(k, 0, below, 0)
        else:
            for line in range(at):
                take_down(k, line, 1, line)
                add_down(k, line, 1)
                pass_down(k, line, 1, line)

    def add_near(k):
        for at in range(1, last):

            @pl.when(z == at)
            def _():
                (rising if low(at) else falling)(k, at)

    def add_far(k):
        for at in range(1, last):

            @pl.when(z == at)
            def _():
                (falling if low(at) else rising)(k, at)

    def finish_expr(k):
        for at in range(lines):

            @pl.when(z == at)
            def _():
                own = pl.ds(at * cb, cb)
                total = es[k][own, :]
                if at > 0:
                    if halved(k) and at < middle:
                        take_up(k, at, 1, 1)
                    elif at == last and (halved(k) or whole(k)):
                        take_up(k, at, 1, 0)
                    elif not halved(k) and not whole(k):
                        take_up(k, at, 1, at)
                    total = total + ru[k][own, :]
                if at < last:
                    if halved(k) and at >= middle:
                        take_down(k, at, 1, 1)
                    elif at == 0 and (halved(k) or whole(k)):
                        take_down(k, at, 1, 0)
                    elif not halved(k) and not whole(k):
                        take_down(k, at, 1, at)
                    total = total + rd[k][own, :]
                ge[:, turn_cols(k)] = total

    def probs_gradient(k):
        at = three_turn_cols(k)
        part = product(grad_3[:, at], expr_3[:, at], ((1,), (1,)))
        if k == 0:
            fs[...] = part
        else:
            fs[...] += part

    def slide_of(p, m):
        return pl.ds(pl.multiple_of(p * rows + m * slide_rows, slide_rows), slide_rows)

    def sum_probs_cores():
        for p in mates + (q,):
            fx[p] = fs[slide_of(p, 1 - core), :]
            send(fx.at[p], fy.at[p], fx_s, fx_r.at[p], sibling)

    def return_probs():
        for p in mates:
            arrived(fy.at[p], fx_r.at[p])
            fz[p] = fs[slide_of(p, core), :] + fy[p]
            send(fz.at[p], fr.at[q], f_s, f_r.at[q], mate(p))
        arrived(fy.at[q], fx_r.at[q])
        fr[q] = fs[slide_of(q, core), :] + fy[q]

    def pass_terms():
        for p in mates:
            arrived(l1.at[p], l1_r.at[p])
        l2[z] = (l1[0] + l1[1]) + (l1[2] + l1[3])
        for o in others:
            send(l2.at[z], l2.at[z], l2_s, l2_r.at[z], (o * PLANE + q, core))

    def part_of(slide, m):
        start = slide * slide_rows + m * (slide_rows // 2)
        return pl.ds(pl.multiple_of(start, slide_rows // 2), slide_rows // 2)

    def finish_logits():
        arrived(inn.at[1 - core], in_r)
        rowv[2] = (inn[0] + inn[1]) + rowv[1] * rowv[0]
        for p in mates:
            arrived(fr.at[p], f_r.at[p])
        for m in range(2):

            @pl.loop(0, slide_rows // STEP_ROWS // 2)
            def _(step):
                row_at = (m * (slide_rows // STEP_ROWS // 2) + step) * STEP_ROWS
                at = pl.ds(pl.multiple_of(row_at, STEP_ROWS), STEP_ROWS)
                whole_at = pl.ds(pl.multiple_of(core * slide_rows + row_at, STEP_ROWS), STEP_ROWS)
                by_mass, total_inner = rowv[1, whole_at, 0:1], rowv[2, whole_at, 0:1]
                for p in range(PLANE):
                    for line in range(lines):
                        here, there = pl.ds(line * cb, cb), (line * PLANE + p) * cb
                        grad = fr[p, at, here] + by_mass * weights[:, there : there + cb]
                        glog[whole_at, pl.ds(there, cb)] = pq[p, whole_at, here] * (grad - total_inner)

            here = part_of(core, m)
            send(glog.at[here], glog.at[here], go_s, go_r.at[m], sibling)

    steps = {
        "far": forward_far,
        "near": forward_near,
        "share": share_logits,
        "take": take_probs,
        "whole": gathered,
        "product": forward_product,
        "sum": finish_pred,
        "turn": transpose,
        "plane": sum_plane,
        "line": sum_line,
        "genes": finish_genes,
        "cores": sum_cores,
        "spots": finish_spots,
        "grad": send_grad,
        "terms": send_terms,
        "backward": backward_product,
        "probs": probs_gradient,
        "exchange": sum_probs_cores,
        "return": return_probs,
        "loss": pass_terms,
        "logits": finish_logits,
        "add_near": add_near,
        "add_far": add_far,
        "expr": finish_expr,
    }
    for name, *where in STEPS:
        steps[name](*where)

    for o in others:
        arrived(l2.at[o], l2_r.at[o])
    loss = l2[0]
    for line in range(1, lines):
        loss = loss + l2[line]
    loss_ref[...] = loss[0:1, 0:1] - (inn[0, 0:1, 1:2] + inn[1, 0:1, 1:2])
    for m in range(2):
        arrived(glog.at[part_of(1 - core, m)], go_r.at[m])

    for k in range(chunks):

        @pl.when(z < last)
        def _():
            sent(bb[k].at[block(z)], ou_s.at[k])

        @pl.when(z > 0)
        def _():
            sent(bb[k].at[block(z)], od_s.at[k])

        for at in range(1, last):

            @pl.when(z == at)
            def _():
                sent(bb[k].at[pl.ds(0, at * cb)], fu_s.at[k])
                sent(bb[k].at[pl.ds((at + 1) * cb, (last - at) * cb)], fd_s.at[k])

    for k in range(turns):
        for at in range(lines):

            @pl.when(z == at)
            def _():
                if at < last:
                    sent(es[k].at[pl.ds((at + 1) * cb, (last - at) * cb)], ru_s.at[k])
                if at > 0:
                    sent(es[k].at[pl.ds(0, at * cb)], rd_s.at[k])

    three = pl.ds(0, len(mates))
    sent(ab.at[three, half(0)], a_s)
    sent(ab.at[three, half(0)], a2_s)
    sent(rs.at[three], r_s)
    for k in range(chunks):
        sent(cr[k].at[three], c_s.at[k])
    sent(s1.at[three], s1_s)
    sent(s2.at[pl.ds(0, last)], s2_s)
    sent(ss.at[0], ss_s)
    for k in range(turns):
        sent(ds[k].at[pl.ds(0, len(mates) * rows)], d_s.at[k])
    sent(inn.at[0], in_s)
    sent(l1.at[three], l1_s)
    sent(l2.at[pl.ds(0, last)], l2_s)
    sent(fr.at[three], f_s)
    sent(fx, fx_s)
    sent(glog.at[half(0)], go_s)


def lane_groups(value):
    parts = [value[:, at : at + LANES] for at in range(0, value.shape[1], LANES)]
    return functools.reduce(lambda a, b: a + b, parts)


def grouped(refs, sizes):
    at = 0
    for size in sizes:
        yield refs[at : at + size]
        at += size


def deliver(pred_in, loss_in, glog_in, gexp_in, pred_ref, loss_ref, glog_ref, gexp_ref, sems):
    slides, slide_rows = pred_ref.shape[0], pred_ref.shape[1]
    pairs = [(gexp_in, gexp_ref), (loss_in, loss_ref)]
    for m in range(slides):
        part = pl.ds(m * slide_rows, slide_rows)
        pairs += [(glog_in.at[part], glog_ref.at[m]), (pred_in.at[part], pred_ref.at[m])]
    copies = [pltpu.make_async_copy(src, dst, sems.at[at]) for at, (src, dst) in enumerate(pairs)]
    for copy in copies:
        copy.start()
    for copy in copies:
        copy.wait()


def plane_call(logits, expr, spatial, slide_spots, spot_cells, cell_prior, lines):
    slides, slide_rows, cells = logits.shape
    rows = slides * slide_rows
    cb, genes = expr.shape
    quarter = lines * cb
    spots = PLANE * rows
    chunks, turns = len(FORWARD), len(BACKWARD)
    dma = pltpu.SemaphoreType.DMA
    vmem = pltpu.VMEM
    anywhere = pl.BlockSpec(memory_space=pl.ANY)
    in_vmem = pl.BlockSpec(memory_space=pltpu.VMEM)
    scratch = [
        pltpu.SMEM((slides,), jnp.int32),
        vmem((slides, slide_rows), jnp.int32),
        vmem((1, cells), jnp.int32),
        vmem((rows, cells), F32),
        vmem((PLANE, slide_rows, quarter), F32),
        vmem((rows, genes), F32),
        vmem((cb, genes), F32),
        vmem((PLANE, rows, quarter), F32),
        vmem((PLANE, rows, quarter), F32),
        vmem((PLANE, rows, quarter), F32),
        vmem((spots, 3 * quarter), BF16),
        vmem((quarter, 3 * spots), BF16),
        vmem((quarter, 3 * genes), BF16),
        vmem((3, rows, LANES), F32),
        vmem((PLANE, 8, genes), F32),
        vmem((lines, 8, genes), F32),
        vmem((8, genes), F32),
        vmem((2, rows, LANES), F32),
        vmem((3, rows, LANES), F32),
        vmem((PLANE, 8, rows), F32),
        vmem((spots, 3 * genes), BF16),
        vmem((spots, quarter), F32),
        vmem((PLANE, slide_rows, quarter), F32),
        vmem((PLANE, slide_rows, quarter), F32),
        vmem((PLANE, slide_rows, quarter), F32),
        vmem((PLANE, slide_rows, quarter), F32),
        vmem((2, rows, LANES), F32),
        vmem((PLANE, 8, LANES), F32),
        vmem((lines, 8, LANES), F32),
        dma((2 * slides + 4,)),
        dma((chunks,)),
        dma((chunks,)),
        dma((chunks,)),
        dma((chunks,)),
        dma((chunks,)),
        dma((chunks,)),
        dma((chunks,)),
        dma((chunks,)),
        dma,
        dma((PLANE,)),
        dma,
        dma((PLANE,)),
        dma,
        dma((PLANE,)),
        dma((chunks,)),
        dma((chunks, PLANE)),
        dma,
        dma((2, PLANE)),
        dma,
        dma((2, lines)),
        dma,
        dma,
        dma((turns,)),
        dma((turns, PLANE)),
        dma((turns,)),
        dma((turns, lines)),
        dma((turns,)),
        dma((turns, lines)),
        dma,
        dma((PLANE,)),
        dma,
        dma((PLANE,)),
        dma,
        dma((2,)),
        dma,
        dma,
        dma,
        dma((PLANE,)),
        dma,
        dma((lines,)),
    ]
    for shape, widths in (
        ((quarter,), FORWARD),
        ((spots,), FORWARD),
        ((PLANE, rows), FORWARD),
        ((spots,), BACKWARD),
        ((quarter,), BACKWARD),
        ((quarter,), BACKWARD),
        ((quarter,), BACKWARD),
    ):
        scratch += [vmem(shape + (width,), F32) for width in widths]
    in_hbm = functools.partial(pltpu.with_memory_space_constraint, memory_space=pltpu.HBM)
    in_place = functools.partial(pltpu.with_memory_space_constraint, memory_space=pltpu.VMEM)
    results = pl.pallas_call(
        functools.partial(plane_kernel, lines, FORWARD, BACKWARD),
        out_shape=(
            vmem((rows, genes), F32),
            vmem((1, 1), F32),
            vmem((rows, cells), F32),
            vmem((cb, genes), F32),
        ),
        in_specs=[anywhere] * 6,
        out_specs=(in_vmem,) * 4,
        scratch_shapes=scratch,
        compiler_params=pltpu.CompilerParams(
            collective_id=0, has_side_effects=True, vmem_limit_bytes=48 * 1024 * 1024
        ),
    )(*map(in_hbm, (logits, expr, spatial, slide_spots, spot_cells, cell_prior.reshape(1, cells))))
    pred, loss, grad_logits, grad_expr = pl.pallas_call(
        deliver,
        out_shape=(
            jax.ShapeDtypeStruct((slides, slide_rows, genes), F32),
            jax.ShapeDtypeStruct((1, 1), F32),
            jax.ShapeDtypeStruct((slides, slide_rows, cells), F32),
            jax.ShapeDtypeStruct((cb, genes), F32),
        ),
        in_specs=[anywhere] * 4,
        out_specs=(anywhere,) * 4,
        scratch_shapes=[dma((2 * slides + 2,))],
        compiler_params=pltpu.CompilerParams(vmem_limit_bytes=4 * 1024 * 1024),
    )(*map(in_place, results))
    return pred, loss.reshape(()), grad_logits, grad_expr


def general_plan(logits, expr, spatial, slide_spots, spot_cells, cell_prior):
    place = lax.axis_index("spot")
    side = lax.axis_index("gene")
    rows_all = logits.shape[1]
    cell_rows = expr.shape[0]
    weights = cell_prior.astype(jnp.float32) / fixed_point
    gene_share = (place == 0).astype(jnp.float32)
    row_share = (side == 0).astype(jnp.float32)
    own_weights = lax.dynamic_slice_in_dim(weights, place * cell_rows, cell_rows, 0)
    expr_acc = jnp.zeros((cell_rows, expr.shape[1]), jnp.float32)
    loss_local = jnp.zeros((), jnp.float32)
    pred_list = []
    grad_list = []
    for slide in range(logits.shape[0]):
        logit_rows = logits[slide]
        counted = spot_cells[slide].astype(jnp.float32)
        target = spatial[slide]
        positions = place * rows_all + jnp.arange(rows_all, dtype=jnp.int32)
        valid = (positions < slide_spots[slide]).astype(jnp.float32)
        peak = jnp.max(logit_rows, axis=1, keepdims=True)
        raised = jnp.exp(logit_rows - peak)
        probs = raised / jnp.sum(raised, axis=1, keepdims=True)
        mass = jnp.dot(probs, weights, precision=lax.Precision.HIGHEST)
        blocks = lax.all_to_all(probs, "spot", split_axis=1, concat_axis=0, tiled=True)
        pred = lax.psum_scatter(
            jnp.dot(blocks, expr, precision=lax.Precision.HIGHEST),
            "spot",
            scatter_dimension=0,
            tiled=True,
        )
        gene_dot = jnp.sum(valid[:, None] * pred * target, axis=0)
        gene_pred = jnp.sum(valid[:, None] * pred * pred, axis=0)
        gene_true = jnp.sum(valid[:, None] * target * target, axis=0)
        mass_part = jnp.sum(valid * mass)
        kcell = valid * counted
        cell_part = jnp.sum(kcell)
        spot_dot = jnp.sum(pred * target, axis=1)
        spot_pred = jnp.sum(pred * pred, axis=1)
        spot_true = jnp.sum(target * target, axis=1)
        gene_dot, gene_pred, gene_true, mass_total, cell_total = lax.psum(
            (gene_dot, gene_pred, gene_true, mass_part, cell_part), "spot"
        )
        spot_dot, spot_pred, spot_true = lax.psum((spot_dot, spot_pred, spot_true), "gene")
        gene_inv = lax.rsqrt(gene_pred * gene_true + tiny)
        cos_gene = gene_dot * gene_inv
        spot_inv = lax.rsqrt(spot_pred * spot_true + tiny)
        cos_spot = spot_dot * spot_inv
        share = kcell / cell_total
        scale_count = slide_spots[slide].astype(jnp.float32)
        kl_part = jnp.sum(
            share * (jnp.log(counted) - jnp.log(cell_total) - jnp.log(mass) + jnp.log(mass_total))
        )
        loss_local = loss_local - gene_share * jnp.sum(cos_gene)
        loss_local = loss_local + row_share * (scale_count * kl_part - jnp.sum(valid * cos_spot))
        gene_back = cos_gene * gene_true / (gene_pred * gene_true + tiny)
        spot_back = cos_spot * spot_true / (spot_pred * spot_true + tiny)
        dpred = -valid[:, None] * (
            target * (gene_inv[None, :] + spot_inv[:, None])
            - pred * gene_back[None, :]
            - pred * spot_back[:, None]
        )
        dmass = scale_count * valid * (1.0 / mass_total - share / mass)
        pred_list.append(pred)
        grads_full, mass_full = (
            lax.all_gather(dpred, "spot", axis=0, tiled=True),
            lax.all_gather(dmass, "spot", axis=0, tiled=True),
        )
        dprob_cells = jnp.dot(grads_full, expr.T, precision=lax.Precision.HIGHEST)
        dprob_cells = lax.psum(dprob_cells, "gene")
        expr_acc = expr_acc + lax.dot_general(
            blocks, grads_full, (((0,), (0,)), ((), ())), precision=lax.Precision.HIGHEST
        )
        dprob_cells = dprob_cells + mass_full[:, None] * own_weights[None, :]
        dprob_rows = lax.all_to_all(dprob_cells, "spot", split_axis=0, concat_axis=1, tiled=True)
        inner = jnp.sum(probs * dprob_rows, axis=1, keepdims=True)
        dlogit = probs * (dprob_rows - inner)
        grad_list.append(dlogit)
    loss = lax.psum(loss_local, ("spot", "gene"))
    return (jnp.stack(pred_list), loss, jnp.stack(grad_list), expr_acc)


def solution(mesh):
    places = mesh.shape["spot"]

    def on_device(logits, expr, spatial, slide_spots, spot_cells, cell_prior):
        if places == PLANE * PLANE and mesh.shape["gene"] == 2 and expr.shape[1] == sum(FORWARD):
            return plane_call(
                logits, expr, spatial, slide_spots, spot_cells, cell_prior, places // PLANE
            )
        return general_plan(logits, expr, spatial, slide_spots, spot_cells, cell_prior)

    in_specs = (
        P(None, "spot", None),
        P("spot", "gene"),
        P(None, "spot", "gene"),
        P(),
        P(None, "spot"),
        P(),
    )
    out_specs = (P(None, "spot", "gene"), P(), P(None, "spot", None), P("spot", "gene"))
    return jax.shard_map(
        on_device, mesh=mesh, in_specs=in_specs, out_specs=out_specs, check_vma=False
    )
```

```python
import functools

import jax
import jax.numpy as jnp
from jax import lax
from jax.experimental import pallas as pl
from jax.experimental.pallas import tpu as pltpu
from jax.sharding import PartitionSpec as P

tiny = 1e-06
fixed_point = 16384.0
F32 = jnp.float32
BF16 = jnp.bfloat16
MESH = pl.DeviceIdType.MESH

PLANE = 4
LANES = 128
STEP_ROWS = 16
BLOCK = 32
TALL = 256
FORWARD = (256, 256, 256, 256)
BACKWARD = (128, 128, 256, 256, 256)
SPLIT = 2
LEAD = 2
EARLY = 3
STEPS = (
    ("far", 0),
    ("far", 1),
    ("share",),
    ("near", 0),
    ("take",),
    ("whole", 0),
    ("product", 0),
    ("whole", 1),
    ("near", 1),
    ("product", 1),
    ("far", 2),
    ("far", 3),
    ("sum", 0),
    ("near", 2),
    ("whole", 2),
    ("product", 2),
    ("sum", 1),
    ("near", 3),
    ("whole", 3),
    ("product", 3),
    ("sum", 2),
    ("plane", 0),
    ("sum", 3),
    ("plane", 1),
    ("cores",),
    ("line", 0),
    ("spots",),
    ("genes", 0),
    ("grad", 0),
    ("grad", 1),
    ("turn", 0),
    ("grad", 2),
    ("line", 1),
    ("grad", 3),
    ("turn", 1),
    ("genes", 1),
    ("backward", 0),
    ("backward", 1),
    ("probs", 0),
    ("grad", 4),
    ("probs", 1),
    ("backward", 2),
    ("probs", 2),
    ("terms",),
    ("add_near", 0),
    ("backward", 3),
    ("add_near", 1),
    ("add_far", 0),
    ("probs", 3),
    ("add_near", 2),
    ("backward", 4),
    ("probs", 4),
    ("exchange",),
    ("add_far", 1),
    ("add_near", 3),
    ("left",),
    ("return",),
    ("loss",),
    ("add_far", 2),
    ("expr", 0),
    ("expr", 1),
    ("add_far", 3),
    ("add_near", 4),
    ("expr", 2),
    ("expr", 3),
    ("add_far", 4),
    ("logits",),
    ("expr", 4),
)


def halves(value):
    high = value.astype(BF16)
    return high, (value - high.astype(F32)).astype(BF16)


def threefold(value):
    high, low = halves(value)
    return jnp.concatenate([high, high, low], axis=1)


def product(a, b, contract):
    return lax.dot_general(a, b, (contract, ((), ())), preferred_element_type=F32)


def plane_kernel(lines, forward_widths, backward_widths, *refs):
    chunks, turns = len(forward_widths), len(backward_widths)
    (
        (logits_ref, expr_ref, spatial_ref, count_in, cells_in, prior_in),
        (pr, loss_ref, glog, ge),
        (count_ref, cells_ref, prior_ref, lg, lq, tg, ex, pq, ab, af, probs_3, turned_3, expr_3, sacc, s1, s2, gv, ss, rowv, rs),
        (grad_3, factor, fs, fx, fy, fz, fr, inn, l1, l2),
        (loc, ou_s, ou_r, od_s, od_r, fu_s, fu_r, fd_s, fd_r, a_s, a_r, a2_s, a2_r, r_s, r_r),
        (c_s, c_r, s1_s, s1_r, s2_s, s2_r, ss_s, ss_r, d_s, d_r, ru_s, ru_r, rd_s, rd_r),
        (f_s, f_r, fx_s, fx_r, go_s, go_r, in_s, in_r, l1_s, l1_r, l2_s, l2_r),
        bb,
        cs,
        cr,
        ds,
        es,
        ru,
        rd,
    ) = grouped(refs, (6, 4, 20, 10, 15, 14, 12, chunks, chunks, chunks, turns, turns, turns, turns))
    place = lax.axis_index("spot")
    core = lax.axis_index("gene")
    z = place // PLANE
    q = place % PLANE
    col, row = q % 2, q // 2
    mates = ((1 - row) * 2 + 1 - col, row * 2 + 1 - col, (1 - row) * 2 + col)
    others = tuple((z + step) % lines for step in range(1, lines))
    up, down = (place + PLANE, core), (place - PLANE, core)
    sibling = (place, 1 - core)
    slides, slide_rows = logits_ref.shape[0], logits_ref.shape[1]
    rows = slides * slide_rows
    cb = expr_ref.shape[0]
    genes = expr_ref.shape[1]
    last = lines - 1

    def mate(p):
        return (z * PLANE + p, core)

    def send(src, dst, send_sem, recv_sem, device):
        copy = pltpu.make_async_remote_copy(
            src_ref=src, dst_ref=dst, send_sem=send_sem, recv_sem=recv_sem, device_id=device, device_id_type=MESH
        )
        copy.start()

    def arrived(dst, recv_sem):
        pltpu.make_async_copy(dst, dst, recv_sem).wait()

    sent = arrived

    def cols(k):
        return pl.ds(sum(forward_widths[:k]), forward_widths[k])

    def turn_cols(k):
        return pl.ds(sum(backward_widths[:k]), backward_widths[k])

    def block(index):
        return pl.ds(pl.multiple_of(index * cb, cb), cb)

    def share(index):
        return pl.ds(pl.multiple_of(index * rows, rows), rows)

    def half(index):
        return pl.ds(pl.multiple_of(index * slide_rows, slide_rows), slide_rows)

    small = ((prior_in, prior_ref), (count_in, count_ref), (cells_in, cells_ref))
    pltpu.make_async_copy(expr_ref, ex, loc.at[2 * slides]).start()
    for m in range(slides):
        pltpu.make_async_copy(logits_ref.at[m], lg.at[half(m)], loc.at[m]).start()
    for at, (src, dst) in enumerate(small):
        pltpu.make_async_copy(src, dst, loc.at[2 * slides + 1 + at]).start()
    for m in range(slides):
        pltpu.make_async_copy(spatial_ref.at[m], tg.at[half(m)], loc.at[slides + m]).start()

    barrier = pltpu.get_barrier_semaphore()
    for p in mates:
        pl.semaphore_signal(barrier, inc=1, device_id=mate(p), device_id_type=MESH)
    for o in others:
        pl.semaphore_signal(barrier, inc=1, device_id=(o * PLANE + q, core), device_id_type=MESH)
    pl.semaphore_signal(barrier, inc=1, device_id=sibling, device_id_type=MESH)
    pltpu.make_async_copy(expr_ref, ex, loc.at[2 * slides]).wait()
    for k in range(chunks):
        bb[k][block(z), :] = ex[:, cols(k)]
    for m in range(slides):
        pltpu.make_async_copy(logits_ref.at[m], lg.at[half(m)], loc.at[m]).wait()
    for p in range(PLANE):
        for line in range(lines):
            lq[p, :, pl.ds(line * cb, cb)] = lg[half(core), pl.ds((line * PLANE + p) * cb, cb)]
    pl.semaphore_wait(barrier, len(mates) + len(others) + 1)

    def own_up(k):
        here = bb[k].at[block(z)]
        send(here, here, ou_s.at[k], ou_r.at[k], up)

    def own_down(k):
        here = bb[k].at[block(z)]
        send(here, here, od_s.at[k], od_r.at[k], down)

    def low(at):
        return 2 * at < lines

    for at in range(lines):

        @pl.when(z == at)
        def _():
            for k in range(chunks):
                if at < last and (not low(at) or at == 0 or k < LEAD):
                    own_up(k)
                if at > 0 and (low(at) or at == last or k < LEAD):
                    own_down(k)

    for p in mates:
        send(lq.at[p], ab.at[q, half(core)], a_s, a_r.at[q], mate(p))

    def from_below(k, at):
        arrived(bb[k].at[pl.ds((at - 1) * cb, cb)], ou_r.at[k])
        if at > 1:
            arrived(bb[k].at[pl.ds(0, (at - 1) * cb)], fu_r.at[k])

    def from_above(k, at):
        arrived(bb[k].at[pl.ds((at + 1) * cb, cb)], od_r.at[k])
        if at < last - 1:
            arrived(bb[k].at[pl.ds((at + 2) * cb, (last - 1 - at) * cb)], fd_r.at[k])

    def upward(k, at):
        from_below(k, at)
        here = bb[k].at[pl.ds(0, at * cb)]
        send(here, here, fu_s.at[k], fu_r.at[k], up)

    def downward(k, at):
        from_above(k, at)
        here = bb[k].at[pl.ds((at + 1) * cb, (last - at) * cb)]
        send(here, here, fd_s.at[k], fd_r.at[k], down)

    def forward_far(k):
        for at in range(1, last):

            @pl.when(z == at)
            def _():
                (upward if low(at) else downward)(k, at)
                if k + LEAD < chunks:
                    (own_up if low(at) else own_down)(k + LEAD)

    def forward_near(k):
        for at in range(1, last):

            @pl.when(z == at)
            def _():
                (downward if low(at) else upward)(k, at)

    def gathered(k):
        @pl.when(z == 0)
        def _():
            from_above(k, 0)

        @pl.when(z == last)
        def _():
            from_below(k, last)

    for at, (src, dst) in enumerate(small):
        pltpu.make_async_copy(src, dst, loc.at[2 * slides + 1 + at]).wait()
    weights = prior_ref[...].astype(F32) / fixed_point

    @pl.loop(0, rows // STEP_ROWS)
    def _(step):
        at = pl.ds(pl.multiple_of(step * STEP_ROWS, STEP_ROWS), STEP_ROWS)
        value = lg[at, :]
        peak = jnp.max(value, axis=1, keepdims=True)
        raised = jnp.exp(value - peak)
        scale = 1.0 / jnp.sum(raised, axis=1, keepdims=True)
        probs = raised * scale
        mass_rows = jnp.sum(probs * weights, axis=1, keepdims=True)
        rowv[0, at, :] = jnp.broadcast_to(mass_rows, (STEP_ROWS, LANES))
        rowv[1, at, :] = jnp.broadcast_to(peak, (STEP_ROWS, LANES))
        rowv[2, at, :] = jnp.broadcast_to(scale, (STEP_ROWS, LANES))
        for p in range(PLANE):
            for line in range(lines):
                at_cells = (line * PLANE + p) * cb
                pq[p, at, pl.ds(line * cb, cb)] = probs[:, at_cells : at_cells + cb]

    wide = lax.broadcasted_iota(jnp.int32, (rows, LANES), 1)
    rs[q] = jnp.where(wide == 0, rowv[1], rowv[2]).T[0:8]
    for p in mates:
        send(rs.at[q], rs.at[q], r_s, r_r.at[q], mate(p))

    rid = lax.broadcasted_iota(jnp.int32, (rows, 1), 0)
    first = rid < slide_rows
    position = place * slide_rows + jnp.where(first, rid, rid - slide_rows)
    count = jnp.where(first, count_ref[0], count_ref[1])
    valid = (position < count).astype(F32)
    scale_count = count.astype(F32)
    square = (slide_rows, slide_rows)
    eye = lax.broadcasted_iota(jnp.int32, square, 0) == lax.broadcasted_iota(jnp.int32, square, 1)
    counted = jnp.concatenate(
        [
            jnp.sum(jnp.where(eye, cells_ref[m : m + 1, :].astype(F32), 0.0), axis=1, keepdims=True)
            for m in range(slides)
        ],
        axis=0,
    )
    mass = rowv[0, :, 0:1]
    kcell = valid * counted

    def by_slide(value):
        return [jnp.sum(value[m * slide_rows : (m + 1) * slide_rows], axis=0, keepdims=True) for m in range(slides)]

    mass_parts = by_slide(valid * mass)
    cell_parts = by_slide(kcell)
    lane = lax.broadcasted_iota(jnp.int32, (1, LANES), 1)
    scalars = jnp.zeros((1, LANES), F32)
    for at, value in enumerate(mass_parts + cell_parts):
        scalars = jnp.where(lane == at, value, scalars)
    for m in range(slides):
        pltpu.make_async_copy(spatial_ref.at[m], tg.at[half(m)], loc.at[slides + m]).wait()
    sacc[...] = jnp.zeros_like(sacc)
    s1[q, 3 * slides :, :] = jnp.zeros((8 - 3 * slides, genes), F32)
    s1[q, 3 * slides : 3 * slides + 1, 0:LANES] = scalars

    def share_logits():
        for p in (mates[1], mates[2], mates[0]):
            here = ab.at[p, half(core)]
            arrived(here, a_r.at[p])
            send(here, here, a2_s, a2_r.at[p], sibling)

    def lay_probs(p, at, value):
        af[p, at, :] = value
        there = pl.ds(pl.multiple_of(p * rows + at.start, BLOCK), BLOCK)
        probs_3[there, :] = threefold(value)

    def take_probs():
        in_blocks(0, rows, lambda at: lay_probs(q, at, pq[q, at, :]))
        for p in (mates[1], mates[2], mates[0]):
            arrived(rs.at[p], r_r.at[p])
            arrived(ab.at[p, half(1 - core)], a2_r.at[p])
            rowv[1] = jnp.concatenate([rs[p].T, jnp.zeros((rows, LANES - 8), F32)], axis=1)

            def take(at):
                probs = jnp.exp(ab[p, at, :] - rowv[1, at, 0:1]) * rowv[1, at, 1:2]
                lay_probs(p, at, probs)

            in_blocks(0, rows, take)

    def transpose(part):
        @pl.loop(0, PLANE // 2)
        def _(step):
            p = part * (PLANE // 2) + step
            high, low_part = halves(af[p].T)
            for third, value in enumerate((high, high, low_part)):
                turned_3[:, pl.ds(pl.multiple_of(third * PLANE * rows + p * rows, rows), rows)] = value

    def in_blocks(start, count, body):
        @pl.loop(0, count // BLOCK)
        def _(step):
            body(pl.ds(pl.multiple_of(start + step * BLOCK, BLOCK), BLOCK))

    quarter = lines * cb

    def lay_factor(at, length, width, value):
        high, low_part = halves(value)
        for third, part in enumerate((high, low_part, high)):
            here = pl.ds(pl.multiple_of(third * length + at.start, BLOCK), BLOCK)
            factor[here, 0:width] = part

    def keep_expr(k, at, value):
        start = sum(forward_widths[:k])
        for turn in range(turns):
            origin, width = sum(backward_widths[:turn]), backward_widths[turn]
            lo, hi = max(start, origin), min(start + forward_widths[k], origin + width)
            if lo < hi:
                high, low_part = halves(value[:, lo - start : hi - start])
                for third, part in enumerate((high, low_part, high)):
                    expr_3[at, pl.ds(3 * origin + third * width + lo - origin, hi - lo)] = part

    def three_turn_cols(k):
        return pl.ds(3 * sum(backward_widths[:k]), 3 * backward_widths[k])

    def forward_product(k):
        width = forward_widths[k]

        def lay(at):
            value = bb[k][at, :]
            lay_factor(at, quarter, width, value)
            keep_expr(k, at, value)

        in_blocks(0, quarter, lay)
        if k < chunks - 1:

            @pl.loop(0, PLANE * rows // TALL)
            def _(step):
                tall = pl.ds(pl.multiple_of(step * TALL, TALL), TALL)
                cs[k][tall, :] = product(probs_3[tall, :], factor[0 : 3 * quarter, 0:width], ((1,), (0,)))

            for p in mates:
                pass_pred(k, p)
        else:
            for side, served in ((1 - row, (mates[0], mates[2])), (row, (mates[1],))):
                pair = pl.ds(pl.multiple_of(2 * side * rows, 2 * rows), 2 * rows)
                cs[k][pair, :] = product(probs_3[pair, :], factor[0 : 3 * quarter, 0:width], ((1,), (0,)))
                for p in served:
                    pass_pred(k, p)

    def pass_pred(k, p):
        send(cs[k].at[share(p)], cr[k].at[q], c_s.at[k], c_r.at[k, q], mate(p))

    def finish_pred(k):
        total = cs[k][share(q), :]
        for p in mates:
            arrived(cr[k].at[p], c_r.at[k, p])
            total = total + cr[k][p]
        pr[:, cols(k)] = total
        truth = tg[:, cols(k)]
        for at, value in enumerate((total * truth, total * total, truth * truth)):
            sacc[at] += lane_groups(value)
        kept = valid * total
        stats = by_slide(kept * truth) + by_slide(kept * total) + by_slide(valid * truth * truth)
        s1[q, 0 : 3 * slides, cols(k)] = jnp.concatenate(stats, axis=0)

    early = sum(forward_widths[:EARLY])
    parts = (pl.ds(0, early), pl.ds(early, genes - early))

    def sum_plane(at):
        for p in mates:
            send(s1.at[q, :, parts[at]], s1.at[q, :, parts[at]], s1_s, s1_r.at[at, q], mate(p))

    def sum_line(at):
        for p in mates:
            arrived(s1.at[p, :, parts[at]], s1_r.at[at, p])
        s2[z, :, parts[at]] = (s1[0, :, parts[at]] + s1[1, :, parts[at]]) + (s1[2, :, parts[at]] + s1[3, :, parts[at]])
        for o in others:
            send(s2.at[z, :, parts[at]], s2.at[z, :, parts[at]], s2_s, s2_r.at[at, z], (o * PLANE + q, core))

    kept = {}

    def finish_genes(at):
        for o in others:
            arrived(s2.at[o, :, parts[at]], s2_r.at[at, o])
        total = s2[0, :, parts[at]]
        for line in range(1, lines):
            total = total + s2[line, :, parts[at]]
        gene_dot, gene_pred, gene_true = total[0:2], total[2:4], total[4:6]
        gene_inv = lax.rsqrt(gene_pred * gene_true + tiny)
        cos_gene = gene_dot * gene_inv
        gv[0:2, parts[at]] = gene_inv
        gv[2:4, parts[at]] = cos_gene * gene_true / (gene_pred * gene_true + tiny)
        kept["genes", at] = jnp.sum(jnp.sum(cos_gene, axis=1, keepdims=True), axis=0, keepdims=True)
        if at == 0:
            kept["mass"] = jnp.where(first, total[6:7, 0:1], total[6:7, 1:2])
            kept["cells"] = jnp.where(first, total[6:7, 2:3], total[6:7, 3:4])

    def sum_cores():
        sums = [jnp.sum(sacc[at], axis=1, keepdims=True) for at in range(3)]
        ss[core] = jnp.where(wide == 0, sums[0], jnp.where(wide == 1, sums[1], sums[2]))
        send(ss.at[core], ss.at[core], ss_s, ss_r, sibling)

    def finish_spots():
        arrived(ss.at[1 - core], ss_r)
        spot = ss[0] + ss[1]
        spot_dot, spot_pred, spot_true = spot[:, 0:1], spot[:, 1:2], spot[:, 2:3]
        spot_inv = lax.rsqrt(spot_pred * spot_true + tiny)
        cos_spot = spot_dot * spot_inv
        kept["inverse"], kept["cos"] = spot_inv, cos_spot
        kept["back"] = cos_spot * spot_true / (spot_pred * spot_true + tiny)
        sacc[0] = jnp.zeros_like(sacc[0])

    def send_grad(k):
        spot_inv, spot_back = kept["inverse"], kept["back"]
        pieces = []
        for m in range(slides):
            lo, hi = m * slide_rows, (m + 1) * slide_rows
            truth, guess = tg[lo:hi, turn_cols(k)], pr[lo:hi, turn_cols(k)]
            inverse, back = gv[m : m + 1, turn_cols(k)], gv[2 + m : 3 + m, turn_cols(k)]
            pieces.append(
                -valid[lo:hi]
                * (truth * (inverse + spot_inv[lo:hi]) - guess * back - guess * spot_back[lo:hi])
            )
        grad = jnp.concatenate(pieces, axis=0)
        here = ds[k].at[share(q)]
        here[...] = grad
        for p in mates:
            send(here, here, d_s.at[k], d_r.at[k, q], mate(p))
        sacc[0] += lane_groups(grad * pr[:, turn_cols(k)])

    def send_terms():
        mass_total, cell_total = kept["mass"], kept["cells"]
        portion = kcell / cell_total
        kl_rows = portion * (jnp.log(counted) - jnp.log(cell_total) - jnp.log(mass) + jnp.log(mass_total))
        dmass = scale_count * valid * (1.0 / mass_total - portion / mass)
        terms = jnp.sum(scale_count * kl_rows - valid * kept["cos"], axis=0, keepdims=True)
        l1[q] = jnp.broadcast_to(terms, (8, LANES))
        for p in mates:
            send(l1.at[q], l1.at[q], l1_s, l1_r.at[q], mate(p))
        inner = jnp.sum(sacc[0], axis=1, keepdims=True)
        inn[core] = jnp.where(wide == 0, inner, kept["genes", 0] + kept["genes", 1])
        send(inn.at[core], inn.at[core], in_s, in_r, sibling)
        rowv[1] = jnp.broadcast_to(dmass, (rows, LANES))

    middle = lines // 2

    def backward_product(k):
        for p in mates:
            arrived(ds[k].at[share(p)], d_r.at[k, p])
        width, spots = backward_widths[k], PLANE * rows

        def lay(at):
            value = ds[k][at, :]
            lay_factor(at, spots, width, value)
            grad_3[at, three_turn_cols(k)] = threefold(value)

        in_blocks(0, spots, lay)
        if not halved(k):

            @pl.loop(0, quarter // TALL)
            def _(step):
                tall = pl.ds(pl.multiple_of(step * TALL, TALL), TALL)
                es[k][tall, :] = product(turned_3[tall, :], factor[0 : 3 * spots, 0:width], ((1,), (0,)))

        for turn in range(2):
            if halved(k):
                side = (1 - z // middle) if turn == 0 else z // middle
                pair = pl.ds(pl.multiple_of(side * middle * cb, middle * cb), middle * cb)
                es[k][pair, :] = product(turned_3[pair, :], factor[0 : 3 * spots, 0:width], ((1,), (0,)))

            @pl.when(z == 0)
            def _():
                if halved(k):
                    pass_up(k, middle if turn == 0 else 1, middle if turn == 0 else middle - 1, turn)
                elif whole(k):
                    if turn == 0:
                        pass_up(k, 1, last, 0)
                elif turn == 0:
                    for line in range(last, 0, -1):
                        pass_up(k, line, 1, line)

            @pl.when(z == last)
            def _():
                if halved(k):
                    pass_down(k, 0 if turn == 0 else middle, middle if turn == 0 else middle - 1, turn)
                elif whole(k):
                    if turn == 0:
                        pass_down(k, 0, last, 0)
                elif turn == 0:
                    for line in range(last):
                        pass_down(k, line, 1, line)

    def halved(k):
        return k == 0

    def whole(k):
        return 0 < k < turns - SPLIT

    def pass_up(k, line, count, slot):
        here = pl.ds(line * cb, count * cb)
        send(es[k].at[here], ru[k].at[here], ru_s.at[k], ru_r.at[k, slot], up)

    def pass_down(k, line, count, slot):
        here = pl.ds(line * cb, count * cb)
        send(es[k].at[here], rd[k].at[here], rd_s.at[k], rd_r.at[k, slot], down)

    def take_up(k, line, count, slot):
        arrived(ru[k].at[pl.ds(line * cb, count * cb)], ru_r.at[k, slot])

    def take_down(k, line, count, slot):
        arrived(rd[k].at[pl.ds(line * cb, count * cb)], rd_r.at[k, slot])

    def add_up(k, line, count):
        def add(at):
            es[k][at, :] += ru[k][at, :]

        in_blocks(line * cb, count * cb, add)

    def add_down(k, line, count):
        def add(at):
            es[k][at, :] += rd[k][at, :]

        in_blocks(line * cb, count * cb, add)

    def rising(k, at):
        if halved(k) or whole(k):
            start = middle if halved(k) else at
            take_up(k, start, lines - start, 0)
            above = max(at + 1, start)
            add_up(k, above, lines - above)
            pass_up(k, above, lines - above, 0)
        else:
            for line in range(last, at, -1):
                take_up(k, line, 1, line)
                add_up(k, line, 1)
                pass_up(k, line, 1, line)

    def falling(k, at):
        if halved(k) or whole(k):
            end = middle if halved(k) else at + 1
            take_down(k, 0, end, 0)
            below = min(at, end)
            add_down(k, 0, below)
            pass_down(k, 0, below, 0)
        else:
            for line in range(at):
                take_down(k, line, 1, line)
                add_down(k, line, 1)
                pass_down(k, line, 1, line)

    def add_near(k):
        for at in range(1, last):

            @pl.when(z == at)
            def _():
                (rising if low(at) else falling)(k, at)

    def add_far(k):
        for at in range(1, last):

            @pl.when(z == at)
            def _():
                (falling if low(at) else rising)(k, at)

    def finish_expr(k):
        for at in range(lines):

            @pl.when(z == at)
            def _():
                if at > 0:
                    if halved(k) and at < middle:
                        take_up(k, at, 1, 1)
                    elif at == last and (halved(k) or whole(k)):
                        take_up(k, at, 1, 0)
                    elif not halved(k) and not whole(k):
                        take_up(k, at, 1, at)
                if at < last:
                    if halved(k) and at >= middle:
                        take_down(k, at, 1, 1)
                    elif at == 0 and (halved(k) or whole(k)):
                        take_down(k, at, 1, 0)
                    elif not halved(k) and not whole(k):
                        take_down(k, at, 1, at)

        from_low, from_high = z > 0, z < last

        @pl.loop(0, cb // BLOCK)
        def _(step):
            here = pl.ds(pl.multiple_of(step * BLOCK, BLOCK), BLOCK)
            own = pl.ds(pl.multiple_of(z * cb + step * BLOCK, BLOCK), BLOCK)
            total = es[k][own, :]
            total = total + jnp.where(from_low, ru[k][own, :], 0.0)
            ge[here, turn_cols(k)] = total + jnp.where(from_high, rd[k][own, :], 0.0)

    def probs_gradient(k):
        at = three_turn_cols(k)

        @pl.loop(0, PLANE * rows // TALL)
        def _(step):
            tall = pl.ds(pl.multiple_of(step * TALL, TALL), TALL)
            part = product(grad_3[tall, at], expr_3[:, at], ((1,), (1,)))
            if k == 0:
                fs[tall, :] = part
            else:
                fs[tall, :] += part

    def slide_of(p, m):
        return pl.ds(pl.multiple_of(p * rows + m * slide_rows, slide_rows), slide_rows)

    def sum_probs_cores():
        for p in mates + (q,):
            fx[p] = fs[slide_of(p, 1 - core), :]
            send(fx.at[p], fy.at[p], fx_s, fx_r.at[p], sibling)

    def return_probs():
        for p in mates:
            arrived(fy.at[p], fx_r.at[p])
            fz[p] = fs[slide_of(p, core), :] + fy[p]
            send(fz.at[p], fr.at[q], f_s, f_r.at[q], mate(p))
        arrived(fy.at[q], fx_r.at[q])
        fr[q] = fs[slide_of(q, core), :] + fy[q]

    def pass_terms():
        for p in mates:
            arrived(l1.at[p], l1_r.at[p])
        l2[z] = (l1[0] + l1[1]) + (l1[2] + l1[3])
        for o in others:
            send(l2.at[z], l2.at[z], l2_s, l2_r.at[z], (o * PLANE + q, core))

    def part_of(slide, m):
        start = slide * slide_rows + m * (slide_rows // 2)
        return pl.ds(pl.multiple_of(start, slide_rows // 2), slide_rows // 2)

    def finish_logits():
        arrived(inn.at[1 - core], in_r)
        rowv[2] = (inn[0] + inn[1]) + rowv[1] * rowv[0]
        for p in mates:
            arrived(fr.at[p], f_r.at[p])
        for m in range(2):

            @pl.loop(0, slide_rows // STEP_ROWS // 2)
            def _(step):
                row_at = (m * (slide_rows // STEP_ROWS // 2) + step) * STEP_ROWS
                at = pl.ds(pl.multiple_of(row_at, STEP_ROWS), STEP_ROWS)
                whole_at = pl.ds(pl.multiple_of(core * slide_rows + row_at, STEP_ROWS), STEP_ROWS)
                by_mass, total_inner = rowv[1, whole_at, 0:1], rowv[2, whole_at, 0:1]
                for p in range(PLANE):
                    for line in range(lines):
                        here, there = pl.ds(line * cb, cb), (line * PLANE + p) * cb
                        grad = fr[p, at, here] + by_mass * weights[:, there : there + cb]
                        glog[whole_at, pl.ds(there, cb)] = pq[p, whole_at, here] * (grad - total_inner)

            here = part_of(core, m)
            send(glog.at[here], glog.at[here], go_s, go_r.at[m], sibling)

    def forward_left():
        for k in range(chunks):

            @pl.when(z < last)
            def _():
                sent(bb[k].at[block(z)], ou_s.at[k])

            @pl.when(z > 0)
            def _():
                sent(bb[k].at[block(z)], od_s.at[k])

            for at in range(1, last):

                @pl.when(z == at)
                def _():
                    sent(bb[k].at[pl.ds(0, at * cb)], fu_s.at[k])
                    sent(bb[k].at[pl.ds((at + 1) * cb, (last - at) * cb)], fd_s.at[k])

        three = pl.ds(0, len(mates))
        sent(ab.at[three, half(0)], a_s)
        sent(ab.at[three, half(0)], a2_s)
        sent(rs.at[three], r_s)
        for k in range(chunks):
            sent(cr[k].at[three], c_s.at[k])
        sent(s1.at[three], s1_s)
        sent(s2.at[pl.ds(0, last)], s2_s)
        sent(ss.at[0], ss_s)

    steps = {
        "far": forward_far,
        "near": forward_near,
        "share": share_logits,
        "take": take_probs,
        "whole": gathered,
        "product": forward_product,
        "sum": finish_pred,
        "turn": transpose,
        "plane": sum_plane,
        "line": sum_line,
        "genes": finish_genes,
        "cores": sum_cores,
        "spots": finish_spots,
        "grad": send_grad,
        "terms": send_terms,
        "backward": backward_product,
        "probs": probs_gradient,
        "exchange": sum_probs_cores,
        "return": return_probs,
        "loss": pass_terms,
        "logits": finish_logits,
        "add_near": add_near,
        "add_far": add_far,
        "expr": finish_expr,
        "left": forward_left,
    }
    for name, *where in STEPS:
        steps[name](*where)

    for o in others:
        arrived(l2.at[o], l2_r.at[o])
    loss = l2[0]
    for line in range(1, lines):
        loss = loss + l2[line]
    loss_ref[...] = loss[0:1, 0:1] - (inn[0, 0:1, 1:2] + inn[1, 0:1, 1:2])
    for m in range(2):
        arrived(glog.at[part_of(1 - core, m)], go_r.at[m])

    for k in range(turns):
        for at in range(lines):

            @pl.when(z == at)
            def _():
                if at < last:
                    sent(es[k].at[pl.ds((at + 1) * cb, (last - at) * cb)], ru_s.at[k])
                if at > 0:
                    sent(es[k].at[pl.ds(0, at * cb)], rd_s.at[k])

    three = pl.ds(0, len(mates))
    for k in range(turns):
        sent(ds[k].at[pl.ds(0, len(mates) * rows)], d_s.at[k])
    sent(inn.at[0], in_s)
    sent(l1.at[three], l1_s)
    sent(l2.at[pl.ds(0, last)], l2_s)
    sent(fr.at[three], f_s)
    sent(fx, fx_s)
    sent(glog.at[half(0)], go_s)


def lane_groups(value):
    parts = [value[:, at : at + LANES] for at in range(0, value.shape[1], LANES)]
    return functools.reduce(lambda a, b: a + b, parts)


def grouped(refs, sizes):
    at = 0
    for size in sizes:
        yield refs[at : at + size]
        at += size


def deliver(pred_in, loss_in, glog_in, gexp_in, pred_ref, loss_ref, glog_ref, gexp_ref, sems):
    slides, slide_rows = pred_ref.shape[0], pred_ref.shape[1]
    pairs = [(gexp_in, gexp_ref), (loss_in, loss_ref)]
    for m in range(slides):
        part = pl.ds(m * slide_rows, slide_rows)
        pairs += [(glog_in.at[part], glog_ref.at[m]), (pred_in.at[part], pred_ref.at[m])]
    copies = [pltpu.make_async_copy(src, dst, sems.at[at]) for at, (src, dst) in enumerate(pairs)]
    for copy in copies:
        copy.start()
    for copy in copies:
        copy.wait()


def plane_call(logits, expr, spatial, slide_spots, spot_cells, cell_prior, lines):
    slides, slide_rows, cells = logits.shape
    rows = slides * slide_rows
    cb, genes = expr.shape
    quarter = lines * cb
    spots = PLANE * rows
    chunks, turns = len(FORWARD), len(BACKWARD)
    dma = pltpu.SemaphoreType.DMA
    vmem = pltpu.VMEM
    anywhere = pl.BlockSpec(memory_space=pl.ANY)
    in_vmem = pl.BlockSpec(memory_space=pltpu.VMEM)
    scratch = [
        pltpu.SMEM((slides,), jnp.int32),
        vmem((slides, slide_rows), jnp.int32),
        vmem((1, cells), jnp.int32),
        vmem((rows, cells), F32),
        vmem((PLANE, slide_rows, quarter), F32),
        vmem((rows, genes), F32),
        vmem((cb, genes), F32),
        vmem((PLANE, rows, quarter), F32),
        vmem((PLANE, rows, quarter), F32),
        vmem((PLANE, rows, quarter), F32),
        vmem((spots, 3 * quarter), BF16),
        vmem((quarter, 3 * spots), BF16),
        vmem((quarter, 3 * genes), BF16),
        vmem((3, rows, LANES), F32),
        vmem((PLANE, 8, genes), F32),
        vmem((lines, 8, genes), F32),
        vmem((8, genes), F32),
        vmem((2, rows, LANES), F32),
        vmem((3, rows, LANES), F32),
        vmem((PLANE, 8, rows), F32),
        vmem((spots, 3 * genes), BF16),
        vmem((3 * max(quarter, spots), max(FORWARD + BACKWARD)), BF16),
        vmem((spots, quarter), F32),
        vmem((PLANE, slide_rows, quarter), F32),
        vmem((PLANE, slide_rows, quarter), F32),
        vmem((PLANE, slide_rows, quarter), F32),
        vmem((PLANE, slide_rows, quarter), F32),
        vmem((2, rows, LANES), F32),
        vmem((PLANE, 8, LANES), F32),
        vmem((lines, 8, LANES), F32),
        dma((2 * slides + 4,)),
        dma((chunks,)),
        dma((chunks,)),
        dma((chunks,)),
        dma((chunks,)),
        dma((chunks,)),
        dma((chunks,)),
        dma((chunks,)),
        dma((chunks,)),
        dma,
        dma((PLANE,)),
        dma,
        dma((PLANE,)),
        dma,
        dma((PLANE,)),
        dma((chunks,)),
        dma((chunks, PLANE)),
        dma,
        dma((2, PLANE)),
        dma,
        dma((2, lines)),
        dma,
        dma,
        dma((turns,)),
        dma((turns, PLANE)),
        dma((turns,)),
        dma((turns, lines)),
        dma((turns,)),
        dma((turns, lines)),
        dma,
        dma((PLANE,)),
        dma,
        dma((PLANE,)),
        dma,
        dma((2,)),
        dma,
        dma,
        dma,
        dma((PLANE,)),
        dma,
        dma((lines,)),
    ]
    for shape, widths in (
        ((quarter,), FORWARD),
        ((spots,), FORWARD),
        ((PLANE, rows), FORWARD),
        ((spots,), BACKWARD),
        ((quarter,), BACKWARD),
        ((quarter,), BACKWARD),
        ((quarter,), BACKWARD),
    ):
        scratch += [vmem(shape + (width,), F32) for width in widths]
    in_hbm = functools.partial(pltpu.with_memory_space_constraint, memory_space=pltpu.HBM)
    in_place = functools.partial(pltpu.with_memory_space_constraint, memory_space=pltpu.VMEM)
    results = pl.pallas_call(
        functools.partial(plane_kernel, lines, FORWARD, BACKWARD),
        out_shape=(
            vmem((rows, genes), F32),
            vmem((1, 1), F32),
            vmem((rows, cells), F32),
            vmem((cb, genes), F32),
        ),
        in_specs=[anywhere] * 6,
        out_specs=(in_vmem,) * 4,
        scratch_shapes=scratch,
        compiler_params=pltpu.CompilerParams(
            collective_id=0, has_side_effects=True, vmem_limit_bytes=48 * 1024 * 1024
        ),
    )(*map(in_hbm, (logits, expr, spatial, slide_spots, spot_cells, cell_prior.reshape(1, cells))))
    pred, loss, grad_logits, grad_expr = pl.pallas_call(
        deliver,
        out_shape=(
            jax.ShapeDtypeStruct((slides, slide_rows, genes), F32),
            jax.ShapeDtypeStruct((1, 1), F32),
            jax.ShapeDtypeStruct((slides, slide_rows, cells), F32),
            jax.ShapeDtypeStruct((cb, genes), F32),
        ),
        in_specs=[anywhere] * 4,
        out_specs=(anywhere,) * 4,
        scratch_shapes=[dma((2 * slides + 2,))],
        compiler_params=pltpu.CompilerParams(vmem_limit_bytes=4 * 1024 * 1024),
    )(*map(in_place, results))
    return pred, loss.reshape(()), grad_logits, grad_expr


def general_plan(logits, expr, spatial, slide_spots, spot_cells, cell_prior):
    place = lax.axis_index("spot")
    side = lax.axis_index("gene")
    rows_all = logits.shape[1]
    cell_rows = expr.shape[0]
    weights = cell_prior.astype(jnp.float32) / fixed_point
    gene_share = (place == 0).astype(jnp.float32)
    row_share = (side == 0).astype(jnp.float32)
    own_weights = lax.dynamic_slice_in_dim(weights, place * cell_rows, cell_rows, 0)
    expr_acc = jnp.zeros((cell_rows, expr.shape[1]), jnp.float32)
    loss_local = jnp.zeros((), jnp.float32)
    pred_list = []
    grad_list = []
    for slide in range(logits.shape[0]):
        logit_rows = logits[slide]
        counted = spot_cells[slide].astype(jnp.float32)
        target = spatial[slide]
        positions = place * rows_all + jnp.arange(rows_all, dtype=jnp.int32)
        valid = (positions < slide_spots[slide]).astype(jnp.float32)
        peak = jnp.max(logit_rows, axis=1, keepdims=True)
        raised = jnp.exp(logit_rows - peak)
        probs = raised / jnp.sum(raised, axis=1, keepdims=True)
        mass = jnp.dot(probs, weights, precision=lax.Precision.HIGHEST)
        blocks = lax.all_to_all(probs, "spot", split_axis=1, concat_axis=0, tiled=True)
        pred = lax.psum_scatter(
            jnp.dot(blocks, expr, precision=lax.Precision.HIGHEST),
            "spot",
            scatter_dimension=0,
            tiled=True,
        )
        gene_dot = jnp.sum(valid[:, None] * pred * target, axis=0)
        gene_pred = jnp.sum(valid[:, None] * pred * pred, axis=0)
        gene_true = jnp.sum(valid[:, None] * target * target, axis=0)
        mass_part = jnp.sum(valid * mass)
        kcell = valid * counted
        cell_part = jnp.sum(kcell)
        spot_dot = jnp.sum(pred * target, axis=1)
        spot_pred = jnp.sum(pred * pred, axis=1)
        spot_true = jnp.sum(target * target, axis=1)
        gene_dot, gene_pred, gene_true, mass_total, cell_total = lax.psum(
            (gene_dot, gene_pred, gene_true, mass_part, cell_part), "spot"
        )
        spot_dot, spot_pred, spot_true = lax.psum((spot_dot, spot_pred, spot_true), "gene")
        gene_inv = lax.rsqrt(gene_pred * gene_true + tiny)
        cos_gene = gene_dot * gene_inv
        spot_inv = lax.rsqrt(spot_pred * spot_true + tiny)
        cos_spot = spot_dot * spot_inv
        share = kcell / cell_total
        scale_count = slide_spots[slide].astype(jnp.float32)
        kl_part = jnp.sum(
            share * (jnp.log(counted) - jnp.log(cell_total) - jnp.log(mass) + jnp.log(mass_total))
        )
        loss_local = loss_local - gene_share * jnp.sum(cos_gene)
        loss_local = loss_local + row_share * (scale_count * kl_part - jnp.sum(valid * cos_spot))
        gene_back = cos_gene * gene_true / (gene_pred * gene_true + tiny)
        spot_back = cos_spot * spot_true / (spot_pred * spot_true + tiny)
        dpred = -valid[:, None] * (
            target * (gene_inv[None, :] + spot_inv[:, None])
            - pred * gene_back[None, :]
            - pred * spot_back[:, None]
        )
        dmass = scale_count * valid * (1.0 / mass_total - share / mass)
        pred_list.append(pred)
        grads_full, mass_full = (
            lax.all_gather(dpred, "spot", axis=0, tiled=True),
            lax.all_gather(dmass, "spot", axis=0, tiled=True),
        )
        dprob_cells = jnp.dot(grads_full, expr.T, precision=lax.Precision.HIGHEST)
        dprob_cells = lax.psum(dprob_cells, "gene")
        expr_acc = expr_acc + lax.dot_general(
            blocks, grads_full, (((0,), (0,)), ((), ())), precision=lax.Precision.HIGHEST
        )
        dprob_cells = dprob_cells + mass_full[:, None] * own_weights[None, :]
        dprob_rows = lax.all_to_all(dprob_cells, "spot", split_axis=0, concat_axis=1, tiled=True)
        inner = jnp.sum(probs * dprob_rows, axis=1, keepdims=True)
        dlogit = probs * (dprob_rows - inner)
        grad_list.append(dlogit)
    loss = lax.psum(loss_local, ("spot", "gene"))
    return (jnp.stack(pred_list), loss, jnp.stack(grad_list), expr_acc)


def solution(mesh):
    places = mesh.shape["spot"]

    def on_device(logits, expr, spatial, slide_spots, spot_cells, cell_prior):
        if places == PLANE * PLANE and mesh.shape["gene"] == 2 and expr.shape[1] == sum(FORWARD):
            return plane_call(
                logits, expr, spatial, slide_spots, spot_cells, cell_prior, places // PLANE
            )
        return general_plan(logits, expr, spatial, slide_spots, spot_cells, cell_prior)

    in_specs = (
        P(None, "spot", None),
        P("spot", "gene"),
        P(None, "spot", "gene"),
        P(),
        P(None, "spot"),
        P(),
    )
    out_specs = (P(None, "spot", "gene"), P(), P(None, "spot", None), P("spot", "gene"))
    return jax.shard_map(
        on_device, mesh=mesh, in_specs=in_specs, out_specs=out_specs, check_vma=False
    )
```

```python
import functools

import jax
import jax.numpy as jnp
from jax import lax
from jax.experimental import pallas as pl
from jax.experimental.pallas import tpu as pltpu
from jax.sharding import PartitionSpec as P

tiny = 1e-06
fixed_point = 16384.0
F32 = jnp.float32
BF16 = jnp.bfloat16
MESH = pl.DeviceIdType.MESH

PLANE = 4
LANES = 128
STEP_ROWS = 16
BLOCK = 32
TALL = 256
FORWARD = (256, 256, 256, 256)
BACKWARD = (128, 128, 256, 256, 256)
SPLIT = 2
EARLY = 3
STEPS = (
    ("share",),
    ("near", 0),
    ("take",),
    ("whole", 0),
    ("product", 0),
    ("whole", 1),
    ("near", 1),
    ("product", 1),
    ("sum", 0),
    ("near", 2),
    ("whole", 2),
    ("product", 2),
    ("sum", 1),
    ("near", 3),
    ("whole", 3),
    ("product", 3),
    ("sum", 2),
    ("plane", 0),
    ("sum", 3),
    ("plane", 1),
    ("cores",),
    ("line", 0),
    ("spots",),
    ("genes", 0),
    ("grad", 0),
    ("grad", 1),
    ("turn", 0),
    ("grad", 2),
    ("line", 1),
    ("grad", 3),
    ("turn", 1),
    ("genes", 1),
    ("backward", 0),
    ("backward", 1),
    ("probs", 0),
    ("grad", 4),
    ("probs", 1),
    ("backward", 2),
    ("probs", 2),
    ("terms",),
    ("add_near", 0),
    ("backward", 3),
    ("add_near", 1),
    ("add_far", 0),
    ("probs", 3),
    ("add_near", 2),
    ("backward", 4),
    ("probs", 4),
    ("exchange",),
    ("add_far", 1),
    ("add_near", 3),
    ("left",),
    ("return",),
    ("loss",),
    ("add_far", 2),
    ("expr", 0),
    ("expr", 1),
    ("add_far", 3),
    ("add_near", 4),
    ("expr", 2),
    ("expr", 3),
    ("add_far", 4),
    ("logits",),
    ("expr", 4),
)


def halves(value):
    high = value.astype(BF16)
    return high, (value - high.astype(F32)).astype(BF16)


def threefold(value):
    high, low = halves(value)
    return jnp.concatenate([high, high, low], axis=1)


def product(a, b, contract):
    return lax.dot_general(a, b, (contract, ((), ())), preferred_element_type=F32)


def plane_kernel(lines, forward_widths, backward_widths, *refs):
    chunks, turns = len(forward_widths), len(backward_widths)
    (
        (logits_ref, expr_ref, spatial_ref, count_in, cells_in, prior_in),
        (pr, loss_ref, glog, ge),
        (count_ref, cells_ref, prior_ref, lg, lq, tg, ex, pq, ab, af, probs_3, turned_3, expr_3, sacc, s1, s2, gv, ss, rowv, rs),
        (grad_3, factor, fs, fx, fy, fz, fr, inn, l1, l2),
        (loc, ag_s, ag_r, a_s, a_r, a2_s, a2_r, r_s, r_r),
        (c_s, c_r, s1_s, s1_r, s2_s, s2_r, ss_s, ss_r, d_s, d_r, ru_s, ru_r, rd_s, rd_r),
        (f_s, f_r, fx_s, fx_r, go_s, go_r, in_s, in_r, l1_s, l1_r, l2_s, l2_r),
        bb,
        cs,
        cr,
        ds,
        es,
        ru,
        rd,
    ) = grouped(refs, (6, 4, 20, 10, 9, 14, 12, chunks, chunks, chunks, turns, turns, turns, turns))
    place = lax.axis_index("spot")
    core = lax.axis_index("gene")
    z = place // PLANE
    q = place % PLANE
    col, row = q % 2, q // 2
    mates = ((1 - row) * 2 + 1 - col, row * 2 + 1 - col, (1 - row) * 2 + col)
    others = tuple((z + step) % lines for step in range(1, lines))
    up, down = (place + PLANE, core), (place - PLANE, core)
    sibling = (place, 1 - core)
    slides, slide_rows = logits_ref.shape[0], logits_ref.shape[1]
    rows = slides * slide_rows
    cb = expr_ref.shape[0]
    genes = expr_ref.shape[1]
    last = lines - 1

    def mate(p):
        return (z * PLANE + p, core)

    def send(src, dst, send_sem, recv_sem, device):
        copy = pltpu.make_async_remote_copy(
            src_ref=src, dst_ref=dst, send_sem=send_sem, recv_sem=recv_sem, device_id=device, device_id_type=MESH
        )
        copy.start()

    def arrived(dst, recv_sem):
        pltpu.make_async_copy(dst, dst, recv_sem).wait()

    sent = arrived

    def cols(k):
        return pl.ds(sum(forward_widths[:k]), forward_widths[k])

    def turn_cols(k):
        return pl.ds(sum(backward_widths[:k]), backward_widths[k])

    def block(index):
        return pl.ds(pl.multiple_of(index * cb, cb), cb)

    def share(index):
        return pl.ds(pl.multiple_of(index * rows, rows), rows)

    def half(index):
        return pl.ds(pl.multiple_of(index * slide_rows, slide_rows), slide_rows)

    small = ((prior_in, prior_ref), (count_in, count_ref), (cells_in, cells_ref))
    pltpu.make_async_copy(expr_ref, ex, loc.at[2 * slides]).start()
    for m in range(slides):
        pltpu.make_async_copy(logits_ref.at[m], lg.at[half(m)], loc.at[m]).start()
    for at, (src, dst) in enumerate(small):
        pltpu.make_async_copy(src, dst, loc.at[2 * slides + 1 + at]).start()
    for m in range(slides):
        pltpu.make_async_copy(spatial_ref.at[m], tg.at[half(m)], loc.at[slides + m]).start()

    barrier = pltpu.get_barrier_semaphore()
    for p in mates:
        pl.semaphore_signal(barrier, inc=1, device_id=mate(p), device_id_type=MESH)
    for o in others:
        pl.semaphore_signal(barrier, inc=1, device_id=(o * PLANE + q, core), device_id_type=MESH)
    pl.semaphore_signal(barrier, inc=1, device_id=sibling, device_id_type=MESH)
    pltpu.make_async_copy(expr_ref, ex, loc.at[2 * slides]).wait()
    for k in range(chunks):
        bb[k][block(z), :] = ex[:, cols(k)]
    for m in range(slides):
        pltpu.make_async_copy(logits_ref.at[m], lg.at[half(m)], loc.at[m]).wait()
    for p in range(PLANE):
        for line in range(lines):
            lq[p, :, pl.ds(line * cb, cb)] = lg[half(core), pl.ds((line * PLANE + p) * cb, cb)]
    pl.semaphore_wait(barrier, len(mates) + len(others) + 1)

    middle = lines // 2

    def low(at):
        return at < middle

    def pass_block(k, line, to):
        here = bb[k].at[block(line)]
        send(here, here, ag_s.at[k], ag_r.at[line, k], (to * PLANE + q, core))

    def have_block(k, line):
        arrived(bb[k].at[block(line)], ag_r.at[line, k])

    def send_own(k):
        @pl.when(z == 0)
        def _():
            for to in range(last, 0, -1):
                pass_block(k, 0, to)

        @pl.when(z == last)
        def _():
            for to in range(last):
                pass_block(k, last, to)

        @pl.when((z > 0) & (z < last))
        def _():
            pass_block(k, z, z + 1 - 2 * (z // middle))
            pass_block(k, z, z - 1 + 2 * (z // middle))

    send_own(0)

    for p in mates:
        send(lq.at[p], ab.at[q, half(core)], a_s, a_r.at[q], mate(p))
    for k in range(1, chunks):
        send_own(k)

    def forward_near(k):
        @pl.when((z > 0) & (z < last))
        def _():
            have_block(k, last - z)
            pass_block(k, last - z, last * (z // middle))

    def gathered(k):
        for at in range(lines):

            @pl.when(z == at)
            def _():
                for line in range(lines):
                    if line != at and (at in (0, last) or line in (0, last)):
                        have_block(k, line)

    for at, (src, dst) in enumerate(small):
        pltpu.make_async_copy(src, dst, loc.at[2 * slides + 1 + at]).wait()
    weights = prior_ref[...].astype(F32) / fixed_point

    @pl.loop(0, rows // STEP_ROWS)
    def _(step):
        at = pl.ds(pl.multiple_of(step * STEP_ROWS, STEP_ROWS), STEP_ROWS)
        value = lg[at, :]
        peak = jnp.max(value, axis=1, keepdims=True)
        raised = jnp.exp(value - peak)
        scale = 1.0 / jnp.sum(raised, axis=1, keepdims=True)
        probs = raised * scale
        mass_rows = jnp.sum(probs * weights, axis=1, keepdims=True)
        rowv[0, at, :] = jnp.broadcast_to(mass_rows, (STEP_ROWS, LANES))
        rowv[1, at, :] = jnp.broadcast_to(peak, (STEP_ROWS, LANES))
        rowv[2, at, :] = jnp.broadcast_to(scale, (STEP_ROWS, LANES))
        for p in range(PLANE):
            for line in range(lines):
                at_cells = (line * PLANE + p) * cb
                pq[p, at, pl.ds(line * cb, cb)] = probs[:, at_cells : at_cells + cb]

    wide = lax.broadcasted_iota(jnp.int32, (rows, LANES), 1)
    rs[q] = jnp.where(wide == 0, rowv[1], rowv[2]).T[0:8]
    for p in mates:
        send(rs.at[q], rs.at[q], r_s, r_r.at[q], mate(p))

    rid = lax.broadcasted_iota(jnp.int32, (rows, 1), 0)
    first = rid < slide_rows
    position = place * slide_rows + jnp.where(first, rid, rid - slide_rows)
    count = jnp.where(first, count_ref[0], count_ref[1])
    valid = (position < count).astype(F32)
    scale_count = count.astype(F32)
    square = (slide_rows, slide_rows)
    eye = lax.broadcasted_iota(jnp.int32, square, 0) == lax.broadcasted_iota(jnp.int32, square, 1)
    counted = jnp.concatenate(
        [
            jnp.sum(jnp.where(eye, cells_ref[m : m + 1, :].astype(F32), 0.0), axis=1, keepdims=True)
            for m in range(slides)
        ],
        axis=0,
    )
    mass = rowv[0, :, 0:1]
    kcell = valid * counted

    def by_slide(value):
        return [jnp.sum(value[m * slide_rows : (m + 1) * slide_rows], axis=0, keepdims=True) for m in range(slides)]

    mass_parts = by_slide(valid * mass)
    cell_parts = by_slide(kcell)
    lane = lax.broadcasted_iota(jnp.int32, (1, LANES), 1)
    scalars = jnp.zeros((1, LANES), F32)
    for at, value in enumerate(mass_parts + cell_parts):
        scalars = jnp.where(lane == at, value, scalars)
    for m in range(slides):
        pltpu.make_async_copy(spatial_ref.at[m], tg.at[half(m)], loc.at[slides + m]).wait()
    sacc[...] = jnp.zeros_like(sacc)
    s1[q, 3 * slides :, :] = jnp.zeros((8 - 3 * slides, genes), F32)
    s1[q, 3 * slides : 3 * slides + 1, 0:LANES] = scalars

    def share_logits():
        for p in (mates[1], mates[2], mates[0]):
            here = ab.at[p, half(core)]
            arrived(here, a_r.at[p])
            send(here, here, a2_s, a2_r.at[p], sibling)

    def lay_probs(p, at, value):
        af[p, at, :] = value
        there = pl.ds(pl.multiple_of(p * rows + at.start, BLOCK), BLOCK)
        probs_3[there, :] = threefold(value)

    def take_probs():
        in_blocks(0, rows, lambda at: lay_probs(q, at, pq[q, at, :]))
        for p in (mates[1], mates[2], mates[0]):
            arrived(rs.at[p], r_r.at[p])
            arrived(ab.at[p, half(1 - core)], a2_r.at[p])
            rowv[1] = jnp.concatenate([rs[p].T, jnp.zeros((rows, LANES - 8), F32)], axis=1)

            def take(at):
                probs = jnp.exp(ab[p, at, :] - rowv[1, at, 0:1]) * rowv[1, at, 1:2]
                lay_probs(p, at, probs)

            in_blocks(0, rows, take)

    def transpose(part):
        @pl.loop(0, PLANE // 2)
        def _(step):
            p = part * (PLANE // 2) + step
            high, low_part = halves(af[p].T)
            for third, value in enumerate((high, high, low_part)):
                turned_3[:, pl.ds(pl.multiple_of(third * PLANE * rows + p * rows, rows), rows)] = value

    def in_blocks(start, count, body):
        @pl.loop(0, count // BLOCK)
        def _(step):
            body(pl.ds(pl.multiple_of(start + step * BLOCK, BLOCK), BLOCK))

    quarter = lines * cb

    def lay_factor(at, length, width, value):
        high, low_part = halves(value)
        for third, part in enumerate((high, low_part, high)):
            here = pl.ds(pl.multiple_of(third * length + at.start, BLOCK), BLOCK)
            factor[here, 0:width] = part

    def keep_expr(k, at, value):
        start = sum(forward_widths[:k])
        for turn in range(turns):
            origin, width = sum(backward_widths[:turn]), backward_widths[turn]
            lo, hi = max(start, origin), min(start + forward_widths[k], origin + width)
            if lo < hi:
                high, low_part = halves(value[:, lo - start : hi - start])
                for third, part in enumerate((high, low_part, high)):
                    expr_3[at, pl.ds(3 * origin + third * width + lo - origin, hi - lo)] = part

    def three_turn_cols(k):
        return pl.ds(3 * sum(backward_widths[:k]), 3 * backward_widths[k])

    def forward_product(k):
        width = forward_widths[k]

        def lay(at):
            value = bb[k][at, :]
            lay_factor(at, quarter, width, value)
            keep_expr(k, at, value)

        in_blocks(0, quarter, lay)
        if k < chunks - 1:

            @pl.loop(0, PLANE * rows // TALL)
            def _(step):
                tall = pl.ds(pl.multiple_of(step * TALL, TALL), TALL)
                cs[k][tall, :] = product(probs_3[tall, :], factor[0 : 3 * quarter, 0:width], ((1,), (0,)))

            for p in mates:
                pass_pred(k, p)
        else:
            for side, served in ((1 - row, (mates[0], mates[2])), (row, (mates[1],))):
                pair = pl.ds(pl.multiple_of(2 * side * rows, 2 * rows), 2 * rows)
                cs[k][pair, :] = product(probs_3[pair, :], factor[0 : 3 * quarter, 0:width], ((1,), (0,)))
                for p in served:
                    pass_pred(k, p)

    def pass_pred(k, p):
        send(cs[k].at[share(p)], cr[k].at[q], c_s.at[k], c_r.at[k, q], mate(p))

    def finish_pred(k):
        total = cs[k][share(q), :]
        for p in mates:
            arrived(cr[k].at[p], c_r.at[k, p])
            total = total + cr[k][p]
        pr[:, cols(k)] = total
        truth = tg[:, cols(k)]
        for at, value in enumerate((total * truth, total * total, truth * truth)):
            sacc[at] += lane_groups(value)
        kept = valid * total
        stats = by_slide(kept * truth) + by_slide(kept * total) + by_slide(valid * truth * truth)
        s1[q, 0 : 3 * slides, cols(k)] = jnp.concatenate(stats, axis=0)

    early = sum(forward_widths[:EARLY])
    parts = (pl.ds(0, early), pl.ds(early, genes - early))

    def sum_plane(at):
        for p in mates:
            send(s1.at[q, :, parts[at]], s1.at[q, :, parts[at]], s1_s, s1_r.at[at, q], mate(p))

    def sum_line(at):
        for p in mates:
            arrived(s1.at[p, :, parts[at]], s1_r.at[at, p])
        s2[z, :, parts[at]] = (s1[0, :, parts[at]] + s1[1, :, parts[at]]) + (s1[2, :, parts[at]] + s1[3, :, parts[at]])
        for o in others:
            send(s2.at[z, :, parts[at]], s2.at[z, :, parts[at]], s2_s, s2_r.at[at, z], (o * PLANE + q, core))

    kept = {}

    def finish_genes(at):
        for o in others:
            arrived(s2.at[o, :, parts[at]], s2_r.at[at, o])
        total = s2[0, :, parts[at]]
        for line in range(1, lines):
            total = total + s2[line, :, parts[at]]
        gene_dot, gene_pred, gene_true = total[0:2], total[2:4], total[4:6]
        gene_inv = lax.rsqrt(gene_pred * gene_true + tiny)
        cos_gene = gene_dot * gene_inv
        gv[0:2, parts[at]] = gene_inv
        gv[2:4, parts[at]] = cos_gene * gene_true / (gene_pred * gene_true + tiny)
        kept["genes", at] = jnp.sum(jnp.sum(cos_gene, axis=1, keepdims=True), axis=0, keepdims=True)
        if at == 0:
            kept["mass"] = jnp.where(first, total[6:7, 0:1], total[6:7, 1:2])
            kept["cells"] = jnp.where(first, total[6:7, 2:3], total[6:7, 3:4])

    def sum_cores():
        sums = [jnp.sum(sacc[at], axis=1, keepdims=True) for at in range(3)]
        ss[core] = jnp.where(wide == 0, sums[0], jnp.where(wide == 1, sums[1], sums[2]))
        send(ss.at[core], ss.at[core], ss_s, ss_r, sibling)

    def finish_spots():
        arrived(ss.at[1 - core], ss_r)
        spot = ss[0] + ss[1]
        spot_dot, spot_pred, spot_true = spot[:, 0:1], spot[:, 1:2], spot[:, 2:3]
        spot_inv = lax.rsqrt(spot_pred * spot_true + tiny)
        cos_spot = spot_dot * spot_inv
        kept["inverse"], kept["cos"] = spot_inv, cos_spot
        kept["back"] = cos_spot * spot_true / (spot_pred * spot_true + tiny)
        sacc[0] = jnp.zeros_like(sacc[0])

    def send_grad(k):
        spot_inv, spot_back = kept["inverse"], kept["back"]
        pieces = []
        for m in range(slides):
            lo, hi = m * slide_rows, (m + 1) * slide_rows
            truth, guess = tg[lo:hi, turn_cols(k)], pr[lo:hi, turn_cols(k)]
            inverse, back = gv[m : m + 1, turn_cols(k)], gv[2 + m : 3 + m, turn_cols(k)]
            pieces.append(
                -valid[lo:hi]
                * (truth * (inverse + spot_inv[lo:hi]) - guess * back - guess * spot_back[lo:hi])
            )
        grad = jnp.concatenate(pieces, axis=0)
        here = ds[k].at[share(q)]
        here[...] = grad
        for p in mates:
            send(here, here, d_s.at[k], d_r.at[k, q], mate(p))
        sacc[0] += lane_groups(grad * pr[:, turn_cols(k)])

    def send_terms():
        mass_total, cell_total = kept["mass"], kept["cells"]
        portion = kcell / cell_total
        kl_rows = portion * (jnp.log(counted) - jnp.log(cell_total) - jnp.log(mass) + jnp.log(mass_total))
        dmass = scale_count * valid * (1.0 / mass_total - portion / mass)
        terms = jnp.sum(scale_count * kl_rows - valid * kept["cos"], axis=0, keepdims=True)
        l1[q] = jnp.broadcast_to(terms, (8, LANES))
        for p in mates:
            send(l1.at[q], l1.at[q], l1_s, l1_r.at[q], mate(p))
        inner = jnp.sum(sacc[0], axis=1, keepdims=True)
        inn[core] = jnp.where(wide == 0, inner, kept["genes", 0] + kept["genes", 1])
        send(inn.at[core], inn.at[core], in_s, in_r, sibling)
        rowv[1] = jnp.broadcast_to(dmass, (rows, LANES))

    def backward_product(k):
        for p in mates:
            arrived(ds[k].at[share(p)], d_r.at[k, p])
        width, spots = backward_widths[k], PLANE * rows

        def lay(at):
            value = ds[k][at, :]
            lay_factor(at, spots, width, value)
            grad_3[at, three_turn_cols(k)] = threefold(value)

        in_blocks(0, spots, lay)
        if not halved(k):

            @pl.loop(0, quarter // TALL)
            def _(step):
                tall = pl.ds(pl.multiple_of(step * TALL, TALL), TALL)
                es[k][tall, :] = product(turned_3[tall, :], factor[0 : 3 * spots, 0:width], ((1,), (0,)))

        for turn in range(2):
            if halved(k):
                side = (1 - z // middle) if turn == 0 else z // middle
                pair = pl.ds(pl.multiple_of(side * middle * cb, middle * cb), middle * cb)
                es[k][pair, :] = product(turned_3[pair, :], factor[0 : 3 * spots, 0:width], ((1,), (0,)))

            @pl.when(z == 0)
            def _():
                if halved(k):
                    pass_up(k, middle if turn == 0 else 1, middle if turn == 0 else middle - 1, turn)
                elif whole(k):
                    if turn == 0:
                        pass_up(k, 1, last, 0)
                elif turn == 0:
                    for line in range(last, 0, -1):
                        pass_up(k, line, 1, line)

            @pl.when(z == last)
            def _():
                if halved(k):
                    pass_down(k, 0 if turn == 0 else middle, middle if turn == 0 else middle - 1, turn)
                elif whole(k):
                    if turn == 0:
                        pass_down(k, 0, last, 0)
                elif turn == 0:
                    for line in range(last):
                        pass_down(k, line, 1, line)

    def halved(k):
        return k == 0

    def whole(k):
        return 0 < k < turns - SPLIT

    def pass_up(k, line, count, slot):
        here = pl.ds(line * cb, count * cb)
        send(es[k].at[here], ru[k].at[here], ru_s.at[k], ru_r.at[k, slot], up)

    def pass_down(k, line, count, slot):
        here = pl.ds(line * cb, count * cb)
        send(es[k].at[here], rd[k].at[here], rd_s.at[k], rd_r.at[k, slot], down)

    def take_up(k, line, count, slot):
        arrived(ru[k].at[pl.ds(line * cb, count * cb)], ru_r.at[k, slot])

    def take_down(k, line, count, slot):
        arrived(rd[k].at[pl.ds(line * cb, count * cb)], rd_r.at[k, slot])

    def add_up(k, line, count):
        def add(at):
            es[k][at, :] += ru[k][at, :]

        in_blocks(line * cb, count * cb, add)

    def add_down(k, line, count):
        def add(at):
            es[k][at, :] += rd[k][at, :]

        in_blocks(line * cb, count * cb, add)

    def rising(k, at):
        if halved(k) or whole(k):
            start = middle if halved(k) else at
            take_up(k, start, lines - start, 0)
            above = max(at + 1, start)
            add_up(k, above, lines - above)
            pass_up(k, above, lines - above, 0)
        else:
            for line in range(last, at, -1):
                take_up(k, line, 1, line)
                add_up(k, line, 1)
                pass_up(k, line, 1, line)

    def falling(k, at):
        if halved(k) or whole(k):
            end = middle if halved(k) else at + 1
            take_down(k, 0, end, 0)
            below = min(at, end)
            add_down(k, 0, below)
            pass_down(k, 0, below, 0)
        else:
            for line in range(at):
                take_down(k, line, 1, line)
                add_down(k, line, 1)
                pass_down(k, line, 1, line)

    def add_near(k):
        for at in range(1, last):

            @pl.when(z == at)
            def _():
                (rising if low(at) else falling)(k, at)

    def add_far(k):
        for at in range(1, last):

            @pl.when(z == at)
            def _():
                (falling if low(at) else rising)(k, at)

    def finish_expr(k):
        for at in range(lines):

            @pl.when(z == at)
            def _():
                if at > 0:
                    if halved(k) and at < middle:
                        take_up(k, at, 1, 1)
                    elif at == last and (halved(k) or whole(k)):
                        take_up(k, at, 1, 0)
                    elif not halved(k) and not whole(k):
                        take_up(k, at, 1, at)
                if at < last:
                    if halved(k) and at >= middle:
                        take_down(k, at, 1, 1)
                    elif at == 0 and (halved(k) or whole(k)):
                        take_down(k, at, 1, 0)
                    elif not halved(k) and not whole(k):
                        take_down(k, at, 1, at)

        from_low, from_high = z > 0, z < last

        @pl.loop(0, cb // BLOCK)
        def _(step):
            here = pl.ds(pl.multiple_of(step * BLOCK, BLOCK), BLOCK)
            own = pl.ds(pl.multiple_of(z * cb + step * BLOCK, BLOCK), BLOCK)
            total = es[k][own, :]
            total = total + jnp.where(from_low, ru[k][own, :], 0.0)
            ge[here, turn_cols(k)] = total + jnp.where(from_high, rd[k][own, :], 0.0)

    def probs_gradient(k):
        at = three_turn_cols(k)

        @pl.loop(0, PLANE * rows // TALL)
        def _(step):
            tall = pl.ds(pl.multiple_of(step * TALL, TALL), TALL)
            part = product(grad_3[tall, at], expr_3[:, at], ((1,), (1,)))
            if k == 0:
                fs[tall, :] = part
            else:
                fs[tall, :] += part

    def slide_of(p, m):
        return pl.ds(pl.multiple_of(p * rows + m * slide_rows, slide_rows), slide_rows)

    def sum_probs_cores():
        for p in mates + (q,):
            fx[p] = fs[slide_of(p, 1 - core), :]
            send(fx.at[p], fy.at[p], fx_s, fx_r.at[p], sibling)

    def return_probs():
        for p in mates:
            arrived(fy.at[p], fx_r.at[p])
            fz[p] = fs[slide_of(p, core), :] + fy[p]
            send(fz.at[p], fr.at[q], f_s, f_r.at[q], mate(p))
        arrived(fy.at[q], fx_r.at[q])
        fr[q] = fs[slide_of(q, core), :] + fy[q]

    def pass_terms():
        for p in mates:
            arrived(l1.at[p], l1_r.at[p])
        l2[z] = (l1[0] + l1[1]) + (l1[2] + l1[3])
        for o in others:
            send(l2.at[z], l2.at[z], l2_s, l2_r.at[z], (o * PLANE + q, core))

    def part_of(slide, m):
        start = slide * slide_rows + m * (slide_rows // 2)
        return pl.ds(pl.multiple_of(start, slide_rows // 2), slide_rows // 2)

    def finish_logits():
        arrived(inn.at[1 - core], in_r)
        rowv[2] = (inn[0] + inn[1]) + rowv[1] * rowv[0]
        for p in mates:
            arrived(fr.at[p], f_r.at[p])
        for m in range(2):

            @pl.loop(0, slide_rows // STEP_ROWS // 2)
            def _(step):
                row_at = (m * (slide_rows // STEP_ROWS // 2) + step) * STEP_ROWS
                at = pl.ds(pl.multiple_of(row_at, STEP_ROWS), STEP_ROWS)
                whole_at = pl.ds(pl.multiple_of(core * slide_rows + row_at, STEP_ROWS), STEP_ROWS)
                by_mass, total_inner = rowv[1, whole_at, 0:1], rowv[2, whole_at, 0:1]
                for p in range(PLANE):
                    for line in range(lines):
                        here, there = pl.ds(line * cb, cb), (line * PLANE + p) * cb
                        grad = fr[p, at, here] + by_mass * weights[:, there : there + cb]
                        glog[whole_at, pl.ds(there, cb)] = pq[p, whole_at, here] * (grad - total_inner)

            here = part_of(core, m)
            send(glog.at[here], glog.at[here], go_s, go_r.at[m], sibling)

    def forward_left():
        for k in range(chunks):
            sent(bb[k].at[pl.ds(0, last * cb)], ag_s.at[k])
        three = pl.ds(0, len(mates))
        sent(ab.at[three, half(0)], a_s)
        sent(ab.at[three, half(0)], a2_s)
        sent(rs.at[three], r_s)
        for k in range(chunks):
            sent(cr[k].at[three], c_s.at[k])
        sent(s1.at[three], s1_s)
        sent(s2.at[pl.ds(0, last)], s2_s)
        sent(ss.at[0], ss_s)

    steps = {
        "near": forward_near,
        "share": share_logits,
        "take": take_probs,
        "whole": gathered,
        "product": forward_product,
        "sum": finish_pred,
        "turn": transpose,
        "plane": sum_plane,
        "line": sum_line,
        "genes": finish_genes,
        "cores": sum_cores,
        "spots": finish_spots,
        "grad": send_grad,
        "terms": send_terms,
        "backward": backward_product,
        "probs": probs_gradient,
        "exchange": sum_probs_cores,
        "return": return_probs,
        "loss": pass_terms,
        "logits": finish_logits,
        "add_near": add_near,
        "add_far": add_far,
        "expr": finish_expr,
        "left": forward_left,
    }
    for name, *where in STEPS:
        steps[name](*where)

    for o in others:
        arrived(l2.at[o], l2_r.at[o])
    loss = l2[0]
    for line in range(1, lines):
        loss = loss + l2[line]
    loss_ref[...] = loss[0:1, 0:1] - (inn[0, 0:1, 1:2] + inn[1, 0:1, 1:2])
    for m in range(2):
        arrived(glog.at[part_of(1 - core, m)], go_r.at[m])

    for k in range(turns):
        for at in range(lines):

            @pl.when(z == at)
            def _():
                if at < last:
                    sent(es[k].at[pl.ds((at + 1) * cb, (last - at) * cb)], ru_s.at[k])
                if at > 0:
                    sent(es[k].at[pl.ds(0, at * cb)], rd_s.at[k])

    three = pl.ds(0, len(mates))
    for k in range(turns):
        sent(ds[k].at[pl.ds(0, len(mates) * rows)], d_s.at[k])
    sent(inn.at[0], in_s)
    sent(l1.at[three], l1_s)
    sent(l2.at[pl.ds(0, last)], l2_s)
    sent(fr.at[three], f_s)
    sent(fx, fx_s)
    sent(glog.at[half(0)], go_s)


def lane_groups(value):
    parts = [value[:, at : at + LANES] for at in range(0, value.shape[1], LANES)]
    return functools.reduce(lambda a, b: a + b, parts)


def grouped(refs, sizes):
    at = 0
    for size in sizes:
        yield refs[at : at + size]
        at += size


def deliver(pred_in, loss_in, glog_in, gexp_in, pred_ref, loss_ref, glog_ref, gexp_ref, sems):
    slides, slide_rows = pred_ref.shape[0], pred_ref.shape[1]
    pairs = [(gexp_in, gexp_ref), (loss_in, loss_ref)]
    for m in range(slides):
        part = pl.ds(m * slide_rows, slide_rows)
        pairs += [(glog_in.at[part], glog_ref.at[m]), (pred_in.at[part], pred_ref.at[m])]
    copies = [pltpu.make_async_copy(src, dst, sems.at[at]) for at, (src, dst) in enumerate(pairs)]
    for copy in copies:
        copy.start()
    for copy in copies:
        copy.wait()


def plane_call(logits, expr, spatial, slide_spots, spot_cells, cell_prior, lines):
    slides, slide_rows, cells = logits.shape
    rows = slides * slide_rows
    cb, genes = expr.shape
    quarter = lines * cb
    spots = PLANE * rows
    chunks, turns = len(FORWARD), len(BACKWARD)
    dma = pltpu.SemaphoreType.DMA
    vmem = pltpu.VMEM
    anywhere = pl.BlockSpec(memory_space=pl.ANY)
    in_vmem = pl.BlockSpec(memory_space=pltpu.VMEM)
    scratch = [
        pltpu.SMEM((slides,), jnp.int32),
        vmem((slides, slide_rows), jnp.int32),
        vmem((1, cells), jnp.int32),
        vmem((rows, cells), F32),
        vmem((PLANE, slide_rows, quarter), F32),
        vmem((rows, genes), F32),
        vmem((cb, genes), F32),
        vmem((PLANE, rows, quarter), F32),
        vmem((PLANE, rows, quarter), F32),
        vmem((PLANE, rows, quarter), F32),
        vmem((spots, 3 * quarter), BF16),
        vmem((quarter, 3 * spots), BF16),
        vmem((quarter, 3 * genes), BF16),
        vmem((3, rows, LANES), F32),
        vmem((PLANE, 8, genes), F32),
        vmem((lines, 8, genes), F32),
        vmem((8, genes), F32),
        vmem((2, rows, LANES), F32),
        vmem((3, rows, LANES), F32),
        vmem((PLANE, 8, rows), F32),
        vmem((spots, 3 * genes), BF16),
        vmem((3 * max(quarter, spots), max(FORWARD + BACKWARD)), BF16),
        vmem((spots, quarter), F32),
        vmem((PLANE, slide_rows, quarter), F32),
        vmem((PLANE, slide_rows, quarter), F32),
        vmem((PLANE, slide_rows, quarter), F32),
        vmem((PLANE, slide_rows, quarter), F32),
        vmem((2, rows, LANES), F32),
        vmem((PLANE, 8, LANES), F32),
        vmem((lines, 8, LANES), F32),
        dma((2 * slides + 4,)),
        dma((chunks,)),
        dma((lines, chunks)),
        dma,
        dma((PLANE,)),
        dma,
        dma((PLANE,)),
        dma,
        dma((PLANE,)),
        dma((chunks,)),
        dma((chunks, PLANE)),
        dma,
        dma((2, PLANE)),
        dma,
        dma((2, lines)),
        dma,
        dma,
        dma((turns,)),
        dma((turns, PLANE)),
        dma((turns,)),
        dma((turns, lines)),
        dma((turns,)),
        dma((turns, lines)),
        dma,
        dma((PLANE,)),
        dma,
        dma((PLANE,)),
        dma,
        dma((2,)),
        dma,
        dma,
        dma,
        dma((PLANE,)),
        dma,
        dma((lines,)),
    ]
    for shape, widths in (
        ((quarter,), FORWARD),
        ((spots,), FORWARD),
        ((PLANE, rows), FORWARD),
        ((spots,), BACKWARD),
        ((quarter,), BACKWARD),
        ((quarter,), BACKWARD),
        ((quarter,), BACKWARD),
    ):
        scratch += [vmem(shape + (width,), F32) for width in widths]
    in_hbm = functools.partial(pltpu.with_memory_space_constraint, memory_space=pltpu.HBM)
    in_place = functools.partial(pltpu.with_memory_space_constraint, memory_space=pltpu.VMEM)
    results = pl.pallas_call(
        functools.partial(plane_kernel, lines, FORWARD, BACKWARD),
        out_shape=(
            vmem((rows, genes), F32),
            vmem((1, 1), F32),
            vmem((rows, cells), F32),
            vmem((cb, genes), F32),
        ),
        in_specs=[anywhere] * 6,
        out_specs=(in_vmem,) * 4,
        scratch_shapes=scratch,
        compiler_params=pltpu.CompilerParams(
            collective_id=0, has_side_effects=True, vmem_limit_bytes=48 * 1024 * 1024
        ),
    )(*map(in_hbm, (logits, expr, spatial, slide_spots, spot_cells, cell_prior.reshape(1, cells))))
    pred, loss, grad_logits, grad_expr = pl.pallas_call(
        deliver,
        out_shape=(
            jax.ShapeDtypeStruct((slides, slide_rows, genes), F32),
            jax.ShapeDtypeStruct((1, 1), F32),
            jax.ShapeDtypeStruct((slides, slide_rows, cells), F32),
            jax.ShapeDtypeStruct((cb, genes), F32),
        ),
        in_specs=[anywhere] * 4,
        out_specs=(anywhere,) * 4,
        scratch_shapes=[dma((2 * slides + 2,))],
        compiler_params=pltpu.CompilerParams(vmem_limit_bytes=4 * 1024 * 1024),
    )(*map(in_place, results))
    return pred, loss.reshape(()), grad_logits, grad_expr


def general_plan(logits, expr, spatial, slide_spots, spot_cells, cell_prior):
    place = lax.axis_index("spot")
    side = lax.axis_index("gene")
    rows_all = logits.shape[1]
    cell_rows = expr.shape[0]
    weights = cell_prior.astype(jnp.float32) / fixed_point
    gene_share = (place == 0).astype(jnp.float32)
    row_share = (side == 0).astype(jnp.float32)
    own_weights = lax.dynamic_slice_in_dim(weights, place * cell_rows, cell_rows, 0)
    expr_acc = jnp.zeros((cell_rows, expr.shape[1]), jnp.float32)
    loss_local = jnp.zeros((), jnp.float32)
    pred_list = []
    grad_list = []
    for slide in range(logits.shape[0]):
        logit_rows = logits[slide]
        counted = spot_cells[slide].astype(jnp.float32)
        target = spatial[slide]
        positions = place * rows_all + jnp.arange(rows_all, dtype=jnp.int32)
        valid = (positions < slide_spots[slide]).astype(jnp.float32)
        peak = jnp.max(logit_rows, axis=1, keepdims=True)
        raised = jnp.exp(logit_rows - peak)
        probs = raised / jnp.sum(raised, axis=1, keepdims=True)
        mass = jnp.dot(probs, weights, precision=lax.Precision.HIGHEST)
        blocks = lax.all_to_all(probs, "spot", split_axis=1, concat_axis=0, tiled=True)
        pred = lax.psum_scatter(
            jnp.dot(blocks, expr, precision=lax.Precision.HIGHEST),
            "spot",
            scatter_dimension=0,
            tiled=True,
        )
        gene_dot = jnp.sum(valid[:, None] * pred * target, axis=0)
        gene_pred = jnp.sum(valid[:, None] * pred * pred, axis=0)
        gene_true = jnp.sum(valid[:, None] * target * target, axis=0)
        mass_part = jnp.sum(valid * mass)
        kcell = valid * counted
        cell_part = jnp.sum(kcell)
        spot_dot = jnp.sum(pred * target, axis=1)
        spot_pred = jnp.sum(pred * pred, axis=1)
        spot_true = jnp.sum(target * target, axis=1)
        gene_dot, gene_pred, gene_true, mass_total, cell_total = lax.psum(
            (gene_dot, gene_pred, gene_true, mass_part, cell_part), "spot"
        )
        spot_dot, spot_pred, spot_true = lax.psum((spot_dot, spot_pred, spot_true), "gene")
        gene_inv = lax.rsqrt(gene_pred * gene_true + tiny)
        cos_gene = gene_dot * gene_inv
        spot_inv = lax.rsqrt(spot_pred * spot_true + tiny)
        cos_spot = spot_dot * spot_inv
        share = kcell / cell_total
        scale_count = slide_spots[slide].astype(jnp.float32)
        kl_part = jnp.sum(
            share * (jnp.log(counted) - jnp.log(cell_total) - jnp.log(mass) + jnp.log(mass_total))
        )
        loss_local = loss_local - gene_share * jnp.sum(cos_gene)
        loss_local = loss_local + row_share * (scale_count * kl_part - jnp.sum(valid * cos_spot))
        gene_back = cos_gene * gene_true / (gene_pred * gene_true + tiny)
        spot_back = cos_spot * spot_true / (spot_pred * spot_true + tiny)
        dpred = -valid[:, None] * (
            target * (gene_inv[None, :] + spot_inv[:, None])
            - pred * gene_back[None, :]
            - pred * spot_back[:, None]
        )
        dmass = scale_count * valid * (1.0 / mass_total - share / mass)
        pred_list.append(pred)
        grads_full, mass_full = (
            lax.all_gather(dpred, "spot", axis=0, tiled=True),
            lax.all_gather(dmass, "spot", axis=0, tiled=True),
        )
        dprob_cells = jnp.dot(grads_full, expr.T, precision=lax.Precision.HIGHEST)
        dprob_cells = lax.psum(dprob_cells, "gene")
        expr_acc = expr_acc + lax.dot_general(
            blocks, grads_full, (((0,), (0,)), ((), ())), precision=lax.Precision.HIGHEST
        )
        dprob_cells = dprob_cells + mass_full[:, None] * own_weights[None, :]
        dprob_rows = lax.all_to_all(dprob_cells, "spot", split_axis=0, concat_axis=1, tiled=True)
        inner = jnp.sum(probs * dprob_rows, axis=1, keepdims=True)
        dlogit = probs * (dprob_rows - inner)
        grad_list.append(dlogit)
    loss = lax.psum(loss_local, ("spot", "gene"))
    return (jnp.stack(pred_list), loss, jnp.stack(grad_list), expr_acc)


def solution(mesh):
    places = mesh.shape["spot"]

    def on_device(logits, expr, spatial, slide_spots, spot_cells, cell_prior):
        if places == PLANE * PLANE and mesh.shape["gene"] == 2 and expr.shape[1] == sum(FORWARD):
            return plane_call(
                logits, expr, spatial, slide_spots, spot_cells, cell_prior, places // PLANE
            )
        return general_plan(logits, expr, spatial, slide_spots, spot_cells, cell_prior)

    in_specs = (
        P(None, "spot", None),
        P("spot", "gene"),
        P(None, "spot", "gene"),
        P(),
        P(None, "spot"),
        P(),
    )
    out_specs = (P(None, "spot", "gene"), P(), P(None, "spot", None), P("spot", "gene"))
    return jax.shard_map(
        on_device, mesh=mesh, in_specs=in_specs, out_specs=out_specs, check_vma=False
    )
```

```python
import functools

import jax
import jax.numpy as jnp
from jax import lax
from jax.experimental import pallas as pl
from jax.experimental.pallas import tpu as pltpu
from jax.sharding import PartitionSpec as P

tiny = 1e-06
fixed_point = 16384.0
F32 = jnp.float32
BF16 = jnp.bfloat16
MESH = pl.DeviceIdType.MESH

PLANE = 4
LANES = 128
STEP_ROWS = 16
BLOCK = 32
TALL = 256
FORWARD = (128, 256, 256, 256, 128)
BACKWARD = (128, 128, 256, 256, 256)
SPLIT = 2
LEAD = 2
NEAR_LEAD = 3
EARLY = 4
STEPS = (
    ("far", 0),
    ("far", 1),
    ("near", 0),
    ("share",),
    ("far", 2),
    ("far", 3),
    ("take",),
    ("whole", 0),
    ("near", 1),
    ("product", 0),
    ("sum", 0),
    ("whole", 1),
    ("near", 2),
    ("product", 1),
    ("whole", 2),
    ("product", 2),
    ("whole", 3),
    ("near", 3),
    ("product", 3),
    ("whole", 4),
    ("far", 4),
    ("near", 4),
    ("turn", 0),
    ("sum", 1),
    ("sum", 2),
    ("product", 4),
    ("turn", 1),
    ("sum", 3),
    ("plane", 0),
    ("sum", 4),
    ("plane", 1),
    ("cores",),
    ("line", 0),
    ("spots",),
    ("genes", 0),
    ("grad", 0),
    ("grad", 1),
    ("grad", 2),
    ("line", 1),
    ("backward", 0),
    ("grad", 3),
    ("backward", 1),
    ("add_near", 0),
    ("genes", 1),
    ("backward", 2),
    ("probs", 0),
    ("add_far", 0),
    ("probs", 1),
    ("expr", 0),
    ("grad", 4),
    ("add_near", 1),
    ("probs", 2),
    ("terms",),
    ("backward", 3),
    ("probs", 3),
    ("add_near", 2),
    ("backward", 4),
    ("add_far", 1),
    ("probs", 4),
    ("exchange",),
    ("add_near", 3),
    ("add_far", 2),
    ("left",),
    ("return",),
    ("loss",),
    ("add_far", 3),
    ("expr", 1),
    ("add_near", 4),
    ("logits",),
    ("add_far", 4),
    ("expr", 2),
    ("expr", 3),
    ("expr", 4),
)


def halves(value):
    high = value.astype(BF16)
    return high, (value - high.astype(F32)).astype(BF16)


def threefold(value):
    high, low = halves(value)
    return jnp.concatenate([high, high, low], axis=1)


def product(a, b, contract):
    return lax.dot_general(a, b, (contract, ((), ())), preferred_element_type=F32)


def plane_kernel(lines, forward_widths, backward_widths, *refs):
    chunks, turns = len(forward_widths), len(backward_widths)
    (
        (logits_ref, expr_ref, spatial_ref, count_in, cells_in, prior_in),
        (pr, loss_ref, glog, ge),
        (count_ref, cells_ref, prior_ref, lg, lq, tg, ex, pq, ab, af, probs_3, turned_3, expr_3, sacc, s1, s2, gv, ss, rowv, rs),
        (grad_3, factor, t0, p0, vr, fs, fx, fy, fz, fr, inn, l1, l2),
        (loc, ou_s, ou_r, od_s, od_r, fu_s, fu_r, fd_s, fd_r, a_s, a_r, a2_s, a2_r, r_s, r_r),
        (c_s, c_r, s1_s, s1_r, s2_s, s2_r, ss_s, ss_r, d_s, d_r, ru_s, ru_r, rd_s, rd_r),
        (f_s, f_r, fx_s, fx_r, go_s, go_r, in_s, in_r, l1_s, l1_r, l2_s, l2_r, t0_s, t0_r, p0_s, p0_r, vr_s, vr_r),
        bb,
        cs,
        cr,
        ds,
        es,
        ru,
        rd,
    ) = grouped(refs, (6, 4, 20, 13, 15, 14, 18, chunks, chunks, chunks, turns, turns, turns, turns))
    place = lax.axis_index("spot")
    core = lax.axis_index("gene")
    z = place // PLANE
    q = place % PLANE
    col, row = q % 2, q // 2
    mates = ((1 - row) * 2 + 1 - col, row * 2 + 1 - col, (1 - row) * 2 + col)
    others = tuple((z + step) % lines for step in range(1, lines))
    up, down = (place + PLANE, core), (place - PLANE, core)
    sibling = (place, 1 - core)
    slides, slide_rows = logits_ref.shape[0], logits_ref.shape[1]
    rows = slides * slide_rows
    cb = expr_ref.shape[0]
    genes = expr_ref.shape[1]
    last = lines - 1

    def mate(p):
        return (z * PLANE + p, core)

    def send(src, dst, send_sem, recv_sem, device):
        copy = pltpu.make_async_remote_copy(
            src_ref=src, dst_ref=dst, send_sem=send_sem, recv_sem=recv_sem, device_id=device, device_id_type=MESH
        )
        copy.start()

    def arrived(dst, recv_sem):
        pltpu.make_async_copy(dst, dst, recv_sem).wait()

    sent = arrived

    def cols(k):
        return pl.ds(sum(forward_widths[:k]), forward_widths[k])

    def turn_cols(k):
        return pl.ds(sum(backward_widths[:k]), backward_widths[k])

    def block(index):
        return pl.ds(pl.multiple_of(index * cb, cb), cb)

    def share(index):
        return pl.ds(pl.multiple_of(index * rows, rows), rows)

    def half(index):
        return pl.ds(pl.multiple_of(index * slide_rows, slide_rows), slide_rows)

    small = ((prior_in, prior_ref), (count_in, count_ref), (cells_in, cells_ref))
    pltpu.make_async_copy(expr_ref, ex, loc.at[2 * slides]).start()
    for m in range(slides):
        pltpu.make_async_copy(logits_ref.at[m], lg.at[half(m)], loc.at[m]).start()
    for at, (src, dst) in enumerate(small):
        pltpu.make_async_copy(src, dst, loc.at[2 * slides + 1 + at]).start()
    for m in range(slides):
        pltpu.make_async_copy(spatial_ref.at[m], tg.at[half(m)], loc.at[slides + m]).start()

    barrier = pltpu.get_barrier_semaphore()
    for p in mates:
        pl.semaphore_signal(barrier, inc=1, device_id=mate(p), device_id_type=MESH)
    for o in others:
        pl.semaphore_signal(barrier, inc=1, device_id=(o * PLANE + q, core), device_id_type=MESH)
    pl.semaphore_signal(barrier, inc=1, device_id=sibling, device_id_type=MESH)
    pltpu.make_async_copy(expr_ref, ex, loc.at[2 * slides]).wait()
    for k in range(chunks):
        bb[k][block(z), :] = ex[:, cols(k)]
    for m in range(slides):
        pltpu.make_async_copy(logits_ref.at[m], lg.at[half(m)], loc.at[m]).wait()
    for p in range(PLANE):
        for line in range(lines):
            lq[p, :, pl.ds(line * cb, cb)] = lg[half(core), pl.ds((line * PLANE + p) * cb, cb)]
    pl.semaphore_wait(barrier, len(mates) + len(others) + 1)

    def own_up(k):
        here = bb[k].at[block(z)]
        send(here, here, ou_s.at[k], ou_r.at[k], up)

    def own_down(k):
        here = bb[k].at[block(z)]
        send(here, here, od_s.at[k], od_r.at[k], down)

    def low(at):
        return 2 * at < lines

    for at in range(lines):

        @pl.when(z == at)
        def _():
            for k in range(chunks):
                if at < last and (at == 0 or k < (LEAD if low(at) else NEAR_LEAD)):
                    own_up(k)
                if at > 0 and (at == last or k < (NEAR_LEAD if low(at) else LEAD)):
                    own_down(k)

    for p in mates:
        send(lq.at[p], ab.at[q, half(core)], a_s, a_r.at[q], mate(p))

    def from_below(k, at):
        arrived(bb[k].at[pl.ds((at - 1) * cb, cb)], ou_r.at[k])
        if at > 1:
            arrived(bb[k].at[pl.ds(0, (at - 1) * cb)], fu_r.at[k])

    def from_above(k, at):
        arrived(bb[k].at[pl.ds((at + 1) * cb, cb)], od_r.at[k])
        if at < last - 1:
            arrived(bb[k].at[pl.ds((at + 2) * cb, (last - 1 - at) * cb)], fd_r.at[k])

    def upward(k, at):
        from_below(k, at)
        here = bb[k].at[pl.ds(0, at * cb)]
        send(here, here, fu_s.at[k], fu_r.at[k], up)

    def downward(k, at):
        from_above(k, at)
        here = bb[k].at[pl.ds((at + 1) * cb, (last - at) * cb)]
        send(here, here, fd_s.at[k], fd_r.at[k], down)

    def forward_far(k):
        for at in range(1, last):

            @pl.when(z == at)
            def _():
                (upward if low(at) else downward)(k, at)
                if k + LEAD < chunks:
                    (own_up if low(at) else own_down)(k + LEAD)

    def forward_near(k):
        for at in range(1, last):

            @pl.when(z == at)
            def _():
                (downward if low(at) else upward)(k, at)
                if k + NEAR_LEAD < chunks:
                    (own_down if low(at) else own_up)(k + NEAR_LEAD)

    def gathered(k):
        @pl.when(z == 0)
        def _():
            from_above(k, 0)

        @pl.when(z == last)
        def _():
            from_below(k, last)

    for at, (src, dst) in enumerate(small):
        pltpu.make_async_copy(src, dst, loc.at[2 * slides + 1 + at]).wait()
    weights = prior_ref[...].astype(F32) / fixed_point

    @pl.loop(0, rows // STEP_ROWS)
    def _(step):
        at = pl.ds(pl.multiple_of(step * STEP_ROWS, STEP_ROWS), STEP_ROWS)
        value = lg[at, :]
        peak = jnp.max(value, axis=1, keepdims=True)
        raised = jnp.exp(value - peak)
        scale = 1.0 / jnp.sum(raised, axis=1, keepdims=True)
        probs = raised * scale
        mass_rows = jnp.sum(probs * weights, axis=1, keepdims=True)
        rowv[0, at, :] = jnp.broadcast_to(mass_rows, (STEP_ROWS, LANES))
        rowv[1, at, :] = jnp.broadcast_to(peak, (STEP_ROWS, LANES))
        rowv[2, at, :] = jnp.broadcast_to(scale, (STEP_ROWS, LANES))
        for p in range(PLANE):
            for line in range(lines):
                at_cells = (line * PLANE + p) * cb
                pq[p, at, pl.ds(line * cb, cb)] = probs[:, at_cells : at_cells + cb]

    wide = lax.broadcasted_iota(jnp.int32, (rows, LANES), 1)
    rs[q] = jnp.where(wide == 0, rowv[1], rowv[2]).T[0:8]
    for p in mates:
        send(rs.at[q], rs.at[q], r_s, r_r.at[q], mate(p))

    rid = lax.broadcasted_iota(jnp.int32, (rows, 1), 0)
    first = rid < slide_rows
    position = place * slide_rows + jnp.where(first, rid, rid - slide_rows)
    count = jnp.where(first, count_ref[0], count_ref[1])
    valid = (position < count).astype(F32)
    scale_count = count.astype(F32)
    square = (slide_rows, slide_rows)
    eye = lax.broadcasted_iota(jnp.int32, square, 0) == lax.broadcasted_iota(jnp.int32, square, 1)
    counted = jnp.concatenate(
        [
            jnp.sum(jnp.where(eye, cells_ref[m : m + 1, :].astype(F32), 0.0), axis=1, keepdims=True)
            for m in range(slides)
        ],
        axis=0,
    )
    mass = rowv[0, :, 0:1]
    kcell = valid * counted

    def by_slide(value):
        return [jnp.sum(value[m * slide_rows : (m + 1) * slide_rows], axis=0, keepdims=True) for m in range(slides)]

    mass_parts = by_slide(valid * mass)
    cell_parts = by_slide(kcell)
    lane = lax.broadcasted_iota(jnp.int32, (1, LANES), 1)
    scalars = jnp.zeros((1, LANES), F32)
    for at, value in enumerate(mass_parts + cell_parts):
        scalars = jnp.where(lane == at, value, scalars)
    for m in range(slides):
        pltpu.make_async_copy(spatial_ref.at[m], tg.at[half(m)], loc.at[slides + m]).wait()

    head = backward_widths[0]
    t0[q] = tg[:, 0:head]
    for p in mates:
        send(t0.at[q], t0.at[q], t0_s, t0_r.at[q], mate(p))
    sacc[...] = jnp.zeros_like(sacc)
    s1[q, 3 * slides :, :] = jnp.zeros((8 - 3 * slides, genes), F32)
    s1[q, 3 * slides : 3 * slides + 1, 0:LANES] = scalars

    def share_logits():
        for p in (mates[1], mates[2], mates[0]):
            here = ab.at[p, half(core)]
            arrived(here, a_r.at[p])
            send(here, here, a2_s, a2_r.at[p], sibling)

    def lay_probs(p, at, value):
        af[p, at, :] = value
        there = pl.ds(pl.multiple_of(p * rows + at.start, BLOCK), BLOCK)
        probs_3[there, :] = threefold(value)

    def take_probs():
        in_blocks(0, rows, lambda at: lay_probs(q, at, pq[q, at, :]))
        for p in (mates[1], mates[2], mates[0]):
            arrived(rs.at[p], r_r.at[p])
            arrived(ab.at[p, half(1 - core)], a2_r.at[p])
            rowv[1] = jnp.concatenate([rs[p].T, jnp.zeros((rows, LANES - 8), F32)], axis=1)

            def take(at):
                probs = jnp.exp(ab[p, at, :] - rowv[1, at, 0:1]) * rowv[1, at, 1:2]
                lay_probs(p, at, probs)

            in_blocks(0, rows, take)

    def transpose(part):
        @pl.loop(0, PLANE // 2)
        def _(step):
            p = part * (PLANE // 2) + step
            high, low_part = halves(af[p].T)
            for third, value in enumerate((high, high, low_part)):
                turned_3[:, pl.ds(pl.multiple_of(third * PLANE * rows + p * rows, rows), rows)] = value

    def in_blocks(start, count, body):
        @pl.loop(0, count // BLOCK)
        def _(step):
            body(pl.ds(pl.multiple_of(start + step * BLOCK, BLOCK), BLOCK))

    quarter = lines * cb

    def lay_factor(at, length, width, value):
        high, low_part = halves(value)
        for third, part in enumerate((high, low_part, high)):
            here = pl.ds(pl.multiple_of(third * length + at.start, BLOCK), BLOCK)
            factor[here, 0:width] = part

    def keep_expr(k, at, value):
        start = sum(forward_widths[:k])
        for turn in range(turns):
            origin, width = sum(backward_widths[:turn]), backward_widths[turn]
            lo, hi = max(start, origin), min(start + forward_widths[k], origin + width)
            if lo < hi:
                high, low_part = halves(value[:, lo - start : hi - start])
                for third, part in enumerate((high, low_part, high)):
                    expr_3[at, pl.ds(3 * origin + third * width + lo - origin, hi - lo)] = part

    def three_turn_cols(k):
        return pl.ds(3 * sum(backward_widths[:k]), 3 * backward_widths[k])

    def forward_product(k):
        width = forward_widths[k]

        def lay(at):
            value = bb[k][at, :]
            lay_factor(at, quarter, width, value)
            keep_expr(k, at, value)

        in_blocks(0, quarter, lay)
        if k < chunks - 1:

            @pl.loop(0, PLANE * rows // TALL)
            def _(step):
                tall = pl.ds(pl.multiple_of(step * TALL, TALL), TALL)
                cs[k][tall, :] = product(probs_3[tall, :], factor[0 : 3 * quarter, 0:width], ((1,), (0,)))

            for p in mates:
                pass_pred(k, p)
        else:
            for side, served in ((1 - row, (mates[0], mates[2])), (row, (mates[1],))):
                pair = pl.ds(pl.multiple_of(2 * side * rows, 2 * rows), 2 * rows)
                cs[k][pair, :] = product(probs_3[pair, :], factor[0 : 3 * quarter, 0:width], ((1,), (0,)))
                for p in served:
                    pass_pred(k, p)

    def pass_pred(k, p):
        send(cs[k].at[share(p)], cr[k].at[q], c_s.at[k], c_r.at[k, q], mate(p))

    def finish_pred(k):
        total = cs[k][share(q), :]
        for p in mates:
            arrived(cr[k].at[p], c_r.at[k, p])
            total = total + cr[k][p]
        pr[:, cols(k)] = total
        if k == 0:
            p0[q] = total[:, 0:head]
            for p in mates:
                send(p0.at[q], p0.at[q], p0_s, p0_r.at[q], mate(p))
        truth = tg[:, cols(k)]
        for at, value in enumerate((total * truth, total * total, truth * truth)):
            sacc[at] += lane_groups(value)
        kept = valid * total
        stats = by_slide(kept * truth) + by_slide(kept * total) + by_slide(valid * truth * truth)
        s1[q, 0 : 3 * slides, cols(k)] = jnp.concatenate(stats, axis=0)

    early = sum(forward_widths[:EARLY])
    parts = (pl.ds(0, early), pl.ds(early, genes - early))

    def sum_plane(at):
        for p in mates:
            send(s1.at[q, :, parts[at]], s1.at[q, :, parts[at]], s1_s, s1_r.at[at, q], mate(p))

    def sum_line(at):
        for p in mates:
            arrived(s1.at[p, :, parts[at]], s1_r.at[at, p])
        s2[z, :, parts[at]] = (s1[0, :, parts[at]] + s1[1, :, parts[at]]) + (s1[2, :, parts[at]] + s1[3, :, parts[at]])
        for o in others:
            send(s2.at[z, :, parts[at]], s2.at[z, :, parts[at]], s2_s, s2_r.at[at, z], (o * PLANE + q, core))

    kept = {}

    def finish_genes(at):
        for o in others:
            arrived(s2.at[o, :, parts[at]], s2_r.at[at, o])
        total = s2[0, :, parts[at]]
        for line in range(1, lines):
            total = total + s2[line, :, parts[at]]
        gene_dot, gene_pred, gene_true = total[0:2], total[2:4], total[4:6]
        gene_inv = lax.rsqrt(gene_pred * gene_true + tiny)
        cos_gene = gene_dot * gene_inv
        gv[0:2, parts[at]] = gene_inv
        gv[2:4, parts[at]] = cos_gene * gene_true / (gene_pred * gene_true + tiny)
        kept["genes", at] = jnp.sum(jnp.sum(cos_gene, axis=1, keepdims=True), axis=0, keepdims=True)
        if at == 0:
            kept["mass"] = jnp.where(first, total[6:7, 0:1], total[6:7, 1:2])
            kept["cells"] = jnp.where(first, total[6:7, 2:3], total[6:7, 3:4])

    def sum_cores():
        sums = [jnp.sum(sacc[at], axis=1, keepdims=True) for at in range(3)]
        ss[core] = jnp.where(wide == 0, sums[0], jnp.where(wide == 1, sums[1], sums[2])).T[0:8]
        send(ss.at[core], ss.at[core], ss_s, ss_r, sibling)

    def finish_spots():
        lane_id = lax.broadcasted_iota(jnp.int32, (1, rows), 1)
        first_lane = lane_id < slide_rows
        lane_position = place * slide_rows + jnp.where(first_lane, lane_id, lane_id - slide_rows)
        lane_valid = (lane_position < jnp.where(first_lane, count_ref[0], count_ref[1])).astype(F32)
        arrived(ss.at[1 - core], ss_r)
        spot = ss[0] + ss[1]
        spot_dot, spot_pred, spot_true = spot[0:1], spot[1:2], spot[2:3]
        spot_inv = lax.rsqrt(spot_pred * spot_true + tiny)
        cos_spot = spot_dot * spot_inv
        spot_back = cos_spot * spot_true / (spot_pred * spot_true + tiny)
        kept["cos"] = jnp.sum(lane_valid * cos_spot, axis=1, keepdims=True)
        vectors = [lane_valid * spot_inv, lane_valid * spot_back, lane_valid, jnp.zeros((5, rows), F32)]
        vr[q] = jnp.concatenate(vectors, axis=0)
        sacc[0] = jnp.zeros_like(sacc[0])

    def gradient(truth, guess, by_row, k):
        pieces = []
        for m in range(slides):
            lo, hi = m * slide_rows, (m + 1) * slide_rows
            inverse, back = gv[m : m + 1, turn_cols(k)], gv[2 + m : 3 + m, turn_cols(k)]
            spot_inv, spot_back, spot_valid = by_row[lo:hi, 0:1], by_row[lo:hi, 1:2], by_row[lo:hi, 2:3]
            pieces.append(
                guess[lo:hi] * (spot_valid * back + spot_back) - truth[lo:hi] * (spot_valid * inverse + spot_inv)
            )
        return jnp.concatenate(pieces, axis=0)

    def head_gradient():
        for p in mates:
            arrived(t0.at[p], t0_r.at[p])
            arrived(p0.at[p], p0_r.at[p])
            arrived(vr.at[p], vr_r.at[p])
        for p in range(PLANE):
            ds[0][share(p), :] = gradient(t0[p], p0[p], vr[p].T, 0)
        sacc[0] += lane_groups(ds[0][share(q), :] * p0[q])

    def send_grad(k):
        if k == 0:
            for p in mates:
                send(vr.at[q], vr.at[q], vr_s, vr_r.at[q], mate(p))
            kept["by_row"] = vr[q].T
            return
        grad = gradient(tg[:, turn_cols(k)], pr[:, turn_cols(k)], kept["by_row"], k)
        here = ds[k].at[share(q)]
        here[...] = grad
        for p in mates:
            send(here, here, d_s.at[k], d_r.at[k, q], mate(p))
        sacc[0] += lane_groups(grad * pr[:, turn_cols(k)])

    def send_terms():
        mass_total, cell_total = kept["mass"], kept["cells"]
        portion = kcell / cell_total
        kl_rows = portion * (jnp.log(counted) - jnp.log(cell_total) - jnp.log(mass) + jnp.log(mass_total))
        dmass = scale_count * valid * (1.0 / mass_total - portion / mass)
        terms = jnp.sum(scale_count * kl_rows, axis=0, keepdims=True) - kept["cos"]
        l1[q] = jnp.broadcast_to(terms, (8, LANES))
        for p in mates:
            send(l1.at[q], l1.at[q], l1_s, l1_r.at[q], mate(p))
        inner = jnp.sum(sacc[0], axis=1, keepdims=True)
        inn[core] = jnp.where(wide == 0, inner, kept["genes", 0] + kept["genes", 1])
        send(inn.at[core], inn.at[core], in_s, in_r, sibling)
        rowv[1] = jnp.broadcast_to(dmass, (rows, LANES))

    middle = lines // 2

    def backward_product(k):
        if k == 0:
            head_gradient()
        else:
            for p in mates:
                arrived(ds[k].at[share(p)], d_r.at[k, p])
        width, spots = backward_widths[k], PLANE * rows

        def lay(at):
            value = ds[k][at, :]
            lay_factor(at, spots, width, value)
            grad_3[at, three_turn_cols(k)] = threefold(value)

        in_blocks(0, spots, lay)
        if not halved(k):

            @pl.loop(0, quarter // TALL)
            def _(step):
                tall = pl.ds(pl.multiple_of(step * TALL, TALL), TALL)
                es[k][tall, :] = product(turned_3[tall, :], factor[0 : 3 * spots, 0:width], ((1,), (0,)))

        for turn in range(2):
            if halved(k):
                side = (1 - z // middle) if turn == 0 else z // middle
                pair = pl.ds(pl.multiple_of(side * middle * cb, middle * cb), middle * cb)
                es[k][pair, :] = product(turned_3[pair, :], factor[0 : 3 * spots, 0:width], ((1,), (0,)))

            @pl.when(z == 0)
            def _():
                if halved(k):
                    pass_up(k, middle if turn == 0 else 1, middle if turn == 0 else middle - 1, turn)
                elif whole(k):
                    if turn == 0:
                        pass_up(k, 1, last, 0)
                elif turn == 0:
                    for line in range(last, 0, -1):
                        pass_up(k, line, 1, line)

            @pl.when(z == last)
            def _():
                if halved(k):
                    pass_down(k, 0 if turn == 0 else middle, middle if turn == 0 else middle - 1, turn)
                elif whole(k):
                    if turn == 0:
                        pass_down(k, 0, last, 0)
                elif turn == 0:
                    for line in range(last):
                        pass_down(k, line, 1, line)

    def halved(k):
        return k == 0

    def whole(k):
        return 0 < k < turns - SPLIT

    def pass_up(k, line, count, slot):
        here = pl.ds(line * cb, count * cb)
        send(es[k].at[here], ru[k].at[here], ru_s.at[k], ru_r.at[k, slot], up)

    def pass_down(k, line, count, slot):
        here = pl.ds(line * cb, count * cb)
        send(es[k].at[here], rd[k].at[here], rd_s.at[k], rd_r.at[k, slot], down)

    def take_up(k, line, count, slot):
        arrived(ru[k].at[pl.ds(line * cb, count * cb)], ru_r.at[k, slot])

    def take_down(k, line, count, slot):
        arrived(rd[k].at[pl.ds(line * cb, count * cb)], rd_r.at[k, slot])

    def add_up(k, line, count):
        def add(at):
            es[k][at, :] += ru[k][at, :]

        in_blocks(line * cb, count * cb, add)

    def add_down(k, line, count):
        def add(at):
            es[k][at, :] += rd[k][at, :]

        in_blocks(line * cb, count * cb, add)

    def rising(k, at):
        if halved(k) or whole(k):
            start = middle if halved(k) else at
            take_up(k, start, lines - start, 0)
            above = max(at + 1, start)
            add_up(k, above, lines - above)
            pass_up(k, above, lines - above, 0)
        else:
            for line in range(last, at, -1):
                take_up(k, line, 1, line)
                add_up(k, line, 1)
                pass_up(k, line, 1, line)

    def falling(k, at):
        if halved(k) or whole(k):
            end = middle if halved(k) else at + 1
            take_down(k, 0, end, 0)
            below = min(at, end)
            add_down(k, 0, below)
            pass_down(k, 0, below, 0)
        else:
            for line in range(at):
                take_down(k, line, 1, line)
                add_down(k, line, 1)
                pass_down(k, line, 1, line)

    def add_near(k):
        for at in range(1, last):

            @pl.when(z == at)
            def _():
                (rising if low(at) else falling)(k, at)

    def add_far(k):
        for at in range(1, last):

            @pl.when(z == at)
            def _():
                (falling if low(at) else rising)(k, at)

    def finish_expr(k):
        for at in range(lines):

            @pl.when(z == at)
            def _():
                if at > 0:
                    if halved(k) and at < middle:
                        take_up(k, at, 1, 1)
                    elif at == last and (halved(k) or whole(k)):
                        take_up(k, at, 1, 0)
                    elif not halved(k) and not whole(k):
                        take_up(k, at, 1, at)
                if at < last:
                    if halved(k) and at >= middle:
                        take_down(k, at, 1, 1)
                    elif at == 0 and (halved(k) or whole(k)):
                        take_down(k, at, 1, 0)
                    elif not halved(k) and not whole(k):
                        take_down(k, at, 1, at)

        from_low, from_high = z > 0, z < last

        @pl.loop(0, cb // BLOCK)
        def _(step):
            here = pl.ds(pl.multiple_of(step * BLOCK, BLOCK), BLOCK)
            own = pl.ds(pl.multiple_of(z * cb + step * BLOCK, BLOCK), BLOCK)
            total = es[k][own, :]
            total = total + jnp.where(from_low, ru[k][own, :], 0.0)
            ge[here, turn_cols(k)] = total + jnp.where(from_high, rd[k][own, :], 0.0)

    def probs_gradient(k):
        at = three_turn_cols(k)

        @pl.loop(0, PLANE * rows // TALL)
        def _(step):
            tall = pl.ds(pl.multiple_of(step * TALL, TALL), TALL)
            part = product(grad_3[tall, at], expr_3[:, at], ((1,), (1,)))
            if k == 0:
                fs[tall, :] = part
            else:
                fs[tall, :] += part

    def slide_of(p, m):
        return pl.ds(pl.multiple_of(p * rows + m * slide_rows, slide_rows), slide_rows)

    def sum_probs_cores():
        for p in mates + (q,):
            fx[p] = fs[slide_of(p, 1 - core), :]
            send(fx.at[p], fy.at[p], fx_s, fx_r.at[p], sibling)

    def return_probs():
        for p in mates:
            arrived(fy.at[p], fx_r.at[p])
            fz[p] = fs[slide_of(p, core), :] + fy[p]
            send(fz.at[p], fr.at[q], f_s, f_r.at[q], mate(p))
        arrived(fy.at[q], fx_r.at[q])
        fr[q] = fs[slide_of(q, core), :] + fy[q]

    def pass_terms():
        for p in mates:
            arrived(l1.at[p], l1_r.at[p])
        l2[z] = (l1[0] + l1[1]) + (l1[2] + l1[3])
        for o in others:
            send(l2.at[z], l2.at[z], l2_s, l2_r.at[z], (o * PLANE + q, core))

    def part_of(slide, m):
        start = slide * slide_rows + m * (slide_rows // 2)
        return pl.ds(pl.multiple_of(start, slide_rows // 2), slide_rows // 2)

    def finish_logits():
        arrived(inn.at[1 - core], in_r)
        rowv[2] = (inn[0] + inn[1]) + rowv[1] * rowv[0]
        for p in mates:
            arrived(fr.at[p], f_r.at[p])
        for m in range(2):

            @pl.loop(0, slide_rows // STEP_ROWS // 2)
            def _(step):
                row_at = (m * (slide_rows // STEP_ROWS // 2) + step) * STEP_ROWS
                at = pl.ds(pl.multiple_of(row_at, STEP_ROWS), STEP_ROWS)
                whole_at = pl.ds(pl.multiple_of(core * slide_rows + row_at, STEP_ROWS), STEP_ROWS)
                by_mass, total_inner = rowv[1, whole_at, 0:1], rowv[2, whole_at, 0:1]
                for p in range(PLANE):
                    for line in range(lines):
                        here, there = pl.ds(line * cb, cb), (line * PLANE + p) * cb
                        grad = fr[p, at, here] + by_mass * weights[:, there : there + cb]
                        glog[whole_at, pl.ds(there, cb)] = pq[p, whole_at, here] * (grad - total_inner)

            here = part_of(core, m)
            send(glog.at[here], glog.at[here], go_s, go_r.at[m], sibling)

    def forward_left():
        for k in range(chunks):

            @pl.when(z < last)
            def _():
                sent(bb[k].at[block(z)], ou_s.at[k])

            @pl.when(z > 0)
            def _():
                sent(bb[k].at[block(z)], od_s.at[k])

            for at in range(1, last):

                @pl.when(z == at)
                def _():
                    sent(bb[k].at[pl.ds(0, at * cb)], fu_s.at[k])
                    sent(bb[k].at[pl.ds((at + 1) * cb, (last - at) * cb)], fd_s.at[k])

        three = pl.ds(0, len(mates))
        sent(ab.at[three, half(0)], a_s)
        sent(ab.at[three, half(0)], a2_s)
        sent(rs.at[three], r_s)
        sent(t0.at[three], t0_s)
        sent(p0.at[three], p0_s)
        for k in range(chunks):
            sent(cr[k].at[three], c_s.at[k])
        sent(s1.at[three], s1_s)
        sent(s2.at[pl.ds(0, last)], s2_s)
        sent(ss.at[0], ss_s)

    steps = {
        "far": forward_far,
        "near": forward_near,
        "share": share_logits,
        "take": take_probs,
        "whole": gathered,
        "product": forward_product,
        "sum": finish_pred,
        "turn": transpose,
        "plane": sum_plane,
        "line": sum_line,
        "genes": finish_genes,
        "cores": sum_cores,
        "spots": finish_spots,
        "grad": send_grad,
        "terms": send_terms,
        "backward": backward_product,
        "probs": probs_gradient,
        "exchange": sum_probs_cores,
        "return": return_probs,
        "loss": pass_terms,
        "logits": finish_logits,
        "add_near": add_near,
        "add_far": add_far,
        "expr": finish_expr,
        "left": forward_left,
    }
    for name, *where in STEPS:
        steps[name](*where)

    for o in others:
        arrived(l2.at[o], l2_r.at[o])
    loss = l2[0]
    for line in range(1, lines):
        loss = loss + l2[line]
    loss_ref[...] = loss[0:1, 0:1] - (inn[0, 0:1, 1:2] + inn[1, 0:1, 1:2])
    for m in range(2):
        arrived(glog.at[part_of(1 - core, m)], go_r.at[m])

    for k in range(turns):
        for at in range(lines):

            @pl.when(z == at)
            def _():
                if at < last:
                    sent(es[k].at[pl.ds((at + 1) * cb, (last - at) * cb)], ru_s.at[k])
                if at > 0:
                    sent(es[k].at[pl.ds(0, at * cb)], rd_s.at[k])

    three = pl.ds(0, len(mates))
    for k in range(1, turns):
        sent(ds[k].at[pl.ds(0, len(mates) * rows)], d_s.at[k])
    sent(vr.at[three], vr_s)
    sent(inn.at[0], in_s)
    sent(l1.at[three], l1_s)
    sent(l2.at[pl.ds(0, last)], l2_s)
    sent(fr.at[three], f_s)
    sent(fx, fx_s)
    sent(glog.at[half(0)], go_s)


def lane_groups(value):
    parts = [value[:, at : at + LANES] for at in range(0, value.shape[1], LANES)]
    return functools.reduce(lambda a, b: a + b, parts)


def grouped(refs, sizes):
    at = 0
    for size in sizes:
        yield refs[at : at + size]
        at += size


def deliver(pred_in, loss_in, glog_in, gexp_in, pred_ref, loss_ref, glog_ref, gexp_ref, sems):
    slides, slide_rows = pred_ref.shape[0], pred_ref.shape[1]
    pairs = [(gexp_in, gexp_ref), (loss_in, loss_ref)]
    for m in range(slides):
        part = pl.ds(m * slide_rows, slide_rows)
        pairs += [(glog_in.at[part], glog_ref.at[m]), (pred_in.at[part], pred_ref.at[m])]
    copies = [pltpu.make_async_copy(src, dst, sems.at[at]) for at, (src, dst) in enumerate(pairs)]
    for copy in copies:
        copy.start()
    for copy in copies:
        copy.wait()


def plane_call(logits, expr, spatial, slide_spots, spot_cells, cell_prior, lines):
    slides, slide_rows, cells = logits.shape
    rows = slides * slide_rows
    cb, genes = expr.shape
    quarter = lines * cb
    spots = PLANE * rows
    chunks, turns = len(FORWARD), len(BACKWARD)
    dma = pltpu.SemaphoreType.DMA
    vmem = pltpu.VMEM
    anywhere = pl.BlockSpec(memory_space=pl.ANY)
    in_vmem = pl.BlockSpec(memory_space=pltpu.VMEM)
    scratch = [
        pltpu.SMEM((slides,), jnp.int32),
        vmem((slides, slide_rows), jnp.int32),
        vmem((1, cells), jnp.int32),
        vmem((rows, cells), F32),
        vmem((PLANE, slide_rows, quarter), F32),
        vmem((rows, genes), F32),
        vmem((cb, genes), F32),
        vmem((PLANE, rows, quarter), F32),
        vmem((PLANE, rows, quarter), F32),
        vmem((PLANE, rows, quarter), F32),
        vmem((spots, 3 * quarter), BF16),
        vmem((quarter, 3 * spots), BF16),
        vmem((quarter, 3 * genes), BF16),
        vmem((3, rows, LANES), F32),
        vmem((PLANE, 8, genes), F32),
        vmem((lines, 8, genes), F32),
        vmem((8, genes), F32),
        vmem((2, 8, rows), F32),
        vmem((3, rows, LANES), F32),
        vmem((PLANE, 8, rows), F32),
        vmem((spots, 3 * genes), BF16),
        vmem((3 * max(quarter, spots), max(FORWARD + BACKWARD)), BF16),
        vmem((PLANE, rows, BACKWARD[0]), F32),
        vmem((PLANE, rows, BACKWARD[0]), F32),
        vmem((PLANE, 8, rows), F32),
        vmem((spots, quarter), F32),
        vmem((PLANE, slide_rows, quarter), F32),
        vmem((PLANE, slide_rows, quarter), F32),
        vmem((PLANE, slide_rows, quarter), F32),
        vmem((PLANE, slide_rows, quarter), F32),
        vmem((2, rows, LANES), F32),
        vmem((PLANE, 8, LANES), F32),
        vmem((lines, 8, LANES), F32),
        dma((2 * slides + 4,)),
        dma((chunks,)),
        dma((chunks,)),
        dma((chunks,)),
        dma((chunks,)),
        dma((chunks,)),
        dma((chunks,)),
        dma((chunks,)),
        dma((chunks,)),
        dma,
        dma((PLANE,)),
        dma,
        dma((PLANE,)),
        dma,
        dma((PLANE,)),
        dma((chunks,)),
        dma((chunks, PLANE)),
        dma,
        dma((2, PLANE)),
        dma,
        dma((2, lines)),
        dma,
        dma,
        dma((turns,)),
        dma((turns, PLANE)),
        dma((turns,)),
        dma((turns, lines)),
        dma((turns,)),
        dma((turns, lines)),
        dma,
        dma((PLANE,)),
        dma,
        dma((PLANE,)),
        dma,
        dma((2,)),
        dma,
        dma,
        dma,
        dma((PLANE,)),
        dma,
        dma((lines,)),
        dma,
        dma((PLANE,)),
        dma,
        dma((PLANE,)),
        dma,
        dma((PLANE,)),
    ]
    for shape, widths in (
        ((quarter,), FORWARD),
        ((spots,), FORWARD),
        ((PLANE, rows), FORWARD),
        ((spots,), BACKWARD),
        ((quarter,), BACKWARD),
        ((quarter,), BACKWARD),
        ((quarter,), BACKWARD),
    ):
        scratch += [vmem(shape + (width,), F32) for width in widths]
    in_hbm = functools.partial(pltpu.with_memory_space_constraint, memory_space=pltpu.HBM)
    in_place = functools.partial(pltpu.with_memory_space_constraint, memory_space=pltpu.VMEM)
    results = pl.pallas_call(
        functools.partial(plane_kernel, lines, FORWARD, BACKWARD),
        out_shape=(
            vmem((rows, genes), F32),
            vmem((1, 1), F32),
            vmem((rows, cells), F32),
            vmem((cb, genes), F32),
        ),
        in_specs=[anywhere] * 6,
        out_specs=(in_vmem,) * 4,
        scratch_shapes=scratch,
        compiler_params=pltpu.CompilerParams(
            collective_id=0, has_side_effects=True, vmem_limit_bytes=48 * 1024 * 1024
        ),
    )(*map(in_hbm, (logits, expr, spatial, slide_spots, spot_cells, cell_prior.reshape(1, cells))))
    pred, loss, grad_logits, grad_expr = pl.pallas_call(
        deliver,
        out_shape=(
            jax.ShapeDtypeStruct((slides, slide_rows, genes), F32),
            jax.ShapeDtypeStruct((1, 1), F32),
            jax.ShapeDtypeStruct((slides, slide_rows, cells), F32),
            jax.ShapeDtypeStruct((cb, genes), F32),
        ),
        in_specs=[anywhere] * 4,
        out_specs=(anywhere,) * 4,
        scratch_shapes=[dma((2 * slides + 2,))],
        compiler_params=pltpu.CompilerParams(vmem_limit_bytes=4 * 1024 * 1024),
    )(*map(in_place, results))
    return pred, loss.reshape(()), grad_logits, grad_expr


def general_plan(logits, expr, spatial, slide_spots, spot_cells, cell_prior):
    place = lax.axis_index("spot")
    side = lax.axis_index("gene")
    rows_all = logits.shape[1]
    cell_rows = expr.shape[0]
    weights = cell_prior.astype(jnp.float32) / fixed_point
    gene_share = (place == 0).astype(jnp.float32)
    row_share = (side == 0).astype(jnp.float32)
    own_weights = lax.dynamic_slice_in_dim(weights, place * cell_rows, cell_rows, 0)
    expr_acc = jnp.zeros((cell_rows, expr.shape[1]), jnp.float32)
    loss_local = jnp.zeros((), jnp.float32)
    pred_list = []
    grad_list = []
    for slide in range(logits.shape[0]):
        logit_rows = logits[slide]
        counted = spot_cells[slide].astype(jnp.float32)
        target = spatial[slide]
        positions = place * rows_all + jnp.arange(rows_all, dtype=jnp.int32)
        valid = (positions < slide_spots[slide]).astype(jnp.float32)
        peak = jnp.max(logit_rows, axis=1, keepdims=True)
        raised = jnp.exp(logit_rows - peak)
        probs = raised / jnp.sum(raised, axis=1, keepdims=True)
        mass = jnp.dot(probs, weights, precision=lax.Precision.HIGHEST)
        blocks = lax.all_to_all(probs, "spot", split_axis=1, concat_axis=0, tiled=True)
        pred = lax.psum_scatter(
            jnp.dot(blocks, expr, precision=lax.Precision.HIGHEST),
            "spot",
            scatter_dimension=0,
            tiled=True,
        )
        gene_dot = jnp.sum(valid[:, None] * pred * target, axis=0)
        gene_pred = jnp.sum(valid[:, None] * pred * pred, axis=0)
        gene_true = jnp.sum(valid[:, None] * target * target, axis=0)
        mass_part = jnp.sum(valid * mass)
        kcell = valid * counted
        cell_part = jnp.sum(kcell)
        spot_dot = jnp.sum(pred * target, axis=1)
        spot_pred = jnp.sum(pred * pred, axis=1)
        spot_true = jnp.sum(target * target, axis=1)
        gene_dot, gene_pred, gene_true, mass_total, cell_total = lax.psum(
            (gene_dot, gene_pred, gene_true, mass_part, cell_part), "spot"
        )
        spot_dot, spot_pred, spot_true = lax.psum((spot_dot, spot_pred, spot_true), "gene")
        gene_inv = lax.rsqrt(gene_pred * gene_true + tiny)
        cos_gene = gene_dot * gene_inv
        spot_inv = lax.rsqrt(spot_pred * spot_true + tiny)
        cos_spot = spot_dot * spot_inv
        share = kcell / cell_total
        scale_count = slide_spots[slide].astype(jnp.float32)
        kl_part = jnp.sum(
            share * (jnp.log(counted) - jnp.log(cell_total) - jnp.log(mass) + jnp.log(mass_total))
        )
        loss_local = loss_local - gene_share * jnp.sum(cos_gene)
        loss_local = loss_local + row_share * (scale_count * kl_part - jnp.sum(valid * cos_spot))
        gene_back = cos_gene * gene_true / (gene_pred * gene_true + tiny)
        spot_back = cos_spot * spot_true / (spot_pred * spot_true + tiny)
        dpred = -valid[:, None] * (
            target * (gene_inv[None, :] + spot_inv[:, None])
            - pred * gene_back[None, :]
            - pred * spot_back[:, None]
        )
        dmass = scale_count * valid * (1.0 / mass_total - share / mass)
        pred_list.append(pred)
        grads_full, mass_full = (
            lax.all_gather(dpred, "spot", axis=0, tiled=True),
            lax.all_gather(dmass, "spot", axis=0, tiled=True),
        )
        dprob_cells = jnp.dot(grads_full, expr.T, precision=lax.Precision.HIGHEST)
        dprob_cells = lax.psum(dprob_cells, "gene")
        expr_acc = expr_acc + lax.dot_general(
            blocks, grads_full, (((0,), (0,)), ((), ())), precision=lax.Precision.HIGHEST
        )
        dprob_cells = dprob_cells + mass_full[:, None] * own_weights[None, :]
        dprob_rows = lax.all_to_all(dprob_cells, "spot", split_axis=0, concat_axis=1, tiled=True)
        inner = jnp.sum(probs * dprob_rows, axis=1, keepdims=True)
        dlogit = probs * (dprob_rows - inner)
        grad_list.append(dlogit)
    loss = lax.psum(loss_local, ("spot", "gene"))
    return (jnp.stack(pred_list), loss, jnp.stack(grad_list), expr_acc)


def solution(mesh):
    places = mesh.shape["spot"]

    def on_device(logits, expr, spatial, slide_spots, spot_cells, cell_prior):
        if places == PLANE * PLANE and mesh.shape["gene"] == 2 and expr.shape[1] == sum(FORWARD):
            return plane_call(
                logits, expr, spatial, slide_spots, spot_cells, cell_prior, places // PLANE
            )
        return general_plan(logits, expr, spatial, slide_spots, spot_cells, cell_prior)

    in_specs = (
        P(None, "spot", None),
        P("spot", "gene"),
        P(None, "spot", "gene"),
        P(),
        P(None, "spot"),
        P(),
    )
    out_specs = (P(None, "spot", "gene"), P(), P(None, "spot", None), P("spot", "gene"))
    return jax.shard_map(
        on_device, mesh=mesh, in_specs=in_specs, out_specs=out_specs, check_vma=False
    )
```

```python
import functools

import jax
import jax.numpy as jnp
from jax import lax
from jax.experimental import pallas as pl
from jax.experimental.pallas import tpu as pltpu
from jax.sharding import PartitionSpec as P

tiny = 1e-06
fixed_point = 16384.0
F32 = jnp.float32
BF16 = jnp.bfloat16
MESH = pl.DeviceIdType.MESH

PLANE = 4
LANES = 128
STEP_ROWS = 16
BLOCK = 32
TALL = 256
FORWARD = (128, 256, 256, 256, 128)
BACKWARD = (128, 128, 256, 256, 256)
SPLIT = 2
LEAD = 2
NEAR_LEAD = 3
EARLY = 3
STEPS = (
    ("far", 0),
    ("far", 1),
    ("share",),
    ("near", 0),
    ("far", 2),
    ("take",),
    ("near", 1),
    ("whole", 0),
    ("far", 3),
    ("product", 0),
    ("near", 2),
    ("sum", 0),
    ("whole", 1),
    ("product", 1),
    ("near", 3),
    ("whole", 2),
    ("far", 4),
    ("near", 4),
    ("product", 2),
    ("turn", 0),
    ("whole", 3),
    ("product", 3),
    ("whole", 4),
    ("sum", 1),
    ("product", 4),
    ("turn", 1),
    ("sum", 2),
    ("plane", 0),
    ("sum", 3),
    ("sum", 4),
    ("plane", 1),
    ("cores",),
    ("line", 0),
    ("genes", 0),
    ("spots",),
    ("grad", 0),
    ("grad", 1),
    ("grad", 2),
    ("backward", 0),
    ("line", 1),
    ("backward", 1),
    ("genes", 1),
    ("add_near", 0),
    ("grad", 3),
    ("probs", 0),
    ("backward", 2),
    ("grad", 4),
    ("probs", 1),
    ("probs", 2),
    ("add_near", 1),
    ("backward", 3),
    ("add_near", 2),
    ("backward", 4),
    ("probs", 3),
    ("probs", 4),
    ("exchange",),
    ("add_near", 3),
    ("add_far", 0),
    ("add_far", 1),
    ("left",),
    ("return",),
    ("expr", 0),
    ("terms",),
    ("expr", 1),
    ("loss",),
    ("add_far", 2),
    ("add_far", 3),
    ("expr", 2),
    ("add_near", 4),
    ("logits",),
    ("add_far", 4),
    ("expr", 3),
    ("expr", 4),
)


def halves(value):
    high = value.astype(BF16)
    return high, (value - high.astype(F32)).astype(BF16)


def threefold(value):
    high, low = halves(value)
    return jnp.concatenate([high, high, low], axis=1)


def product(a, b, contract):
    return lax.dot_general(a, b, (contract, ((), ())), preferred_element_type=F32)


def plane_kernel(lines, forward_widths, backward_widths, *refs):
    chunks, turns = len(forward_widths), len(backward_widths)
    (
        (logits_ref, expr_ref, spatial_ref, count_in, cells_in, prior_in),
        (pr, loss_ref, glog, ge),
        (count_ref, cells_ref, prior_ref, lg, lq, tg, ex, pq, ab, af, probs_3, turned_3, expr_3, sacc, s1, s2, gv, ss, rowv, rs),
        (grad_3, factor, t0, p0, vr, fs, fx, fy, fz, fr, inn, l1, l2),
        (loc, ou_s, ou_r, od_s, od_r, fu_s, fu_r, fd_s, fd_r, a_s, a_r, a2_s, a2_r, r_s, r_r),
        (c_s, c_r, s1_s, s1_r, s2_s, s2_r, ss_s, ss_r, d_s, d_r, ru_s, ru_r, rd_s, rd_r),
        (f_s, f_r, fx_s, fx_r, go_s, go_r, in_s, in_r, l1_s, l1_r, l2_s, l2_r, t0_s, t0_r, p0_s, p0_r),
        bb,
        cs,
        cr,
        ds,
        es,
        ru,
        rd,
    ) = grouped(refs, (6, 4, 20, 13, 15, 14, 16, chunks, chunks, chunks, turns, turns, turns, turns))
    place = lax.axis_index("spot")
    core = lax.axis_index("gene")
    z = place // PLANE
    q = place % PLANE
    col, row = q % 2, q // 2
    mates = ((1 - row) * 2 + 1 - col, row * 2 + 1 - col, (1 - row) * 2 + col)
    others = tuple((z + step) % lines for step in range(1, lines))
    up, down = (place + PLANE, core), (place - PLANE, core)
    sibling = (place, 1 - core)
    slides, slide_rows = logits_ref.shape[0], logits_ref.shape[1]
    rows = slides * slide_rows
    cb = expr_ref.shape[0]
    genes = expr_ref.shape[1]
    last = lines - 1

    def mate(p):
        return (z * PLANE + p, core)

    def across(p):
        return (z * PLANE + p, 1 - core)

    def send(src, dst, send_sem, recv_sem, device):
        copy = pltpu.make_async_remote_copy(
            src_ref=src, dst_ref=dst, send_sem=send_sem, recv_sem=recv_sem, device_id=device, device_id_type=MESH
        )
        copy.start()

    def arrived(dst, recv_sem):
        pltpu.make_async_copy(dst, dst, recv_sem).wait()

    sent = arrived

    def cols(k):
        return pl.ds(sum(forward_widths[:k]), forward_widths[k])

    def turn_cols(k):
        return pl.ds(sum(backward_widths[:k]), backward_widths[k])

    def block(index):
        return pl.ds(pl.multiple_of(index * cb, cb), cb)

    def share(index):
        return pl.ds(pl.multiple_of(index * rows, rows), rows)

    def half(index):
        return pl.ds(pl.multiple_of(index * slide_rows, slide_rows), slide_rows)

    small = ((prior_in, prior_ref), (count_in, count_ref), (cells_in, cells_ref))
    pltpu.make_async_copy(expr_ref, ex, loc.at[2 * slides]).start()
    for m in range(slides):
        pltpu.make_async_copy(logits_ref.at[m], lg.at[half(m)], loc.at[m]).start()
    for at, (src, dst) in enumerate(small):
        pltpu.make_async_copy(src, dst, loc.at[2 * slides + 1 + at]).start()
    for m in range(slides):
        pltpu.make_async_copy(spatial_ref.at[m], tg.at[half(m)], loc.at[slides + m]).start()

    barrier = pltpu.get_barrier_semaphore()
    for p in mates:
        pl.semaphore_signal(barrier, inc=1, device_id=mate(p), device_id_type=MESH)
        pl.semaphore_signal(barrier, inc=1, device_id=across(p), device_id_type=MESH)
    for o in others:
        pl.semaphore_signal(barrier, inc=1, device_id=(o * PLANE + q, core), device_id_type=MESH)
    pl.semaphore_signal(barrier, inc=1, device_id=sibling, device_id_type=MESH)
    pltpu.make_async_copy(expr_ref, ex, loc.at[2 * slides]).wait()
    for k in range(chunks):
        bb[k][block(z), :] = ex[:, cols(k)]
    for m in range(slides):
        pltpu.make_async_copy(logits_ref.at[m], lg.at[half(m)], loc.at[m]).wait()
    for p in range(PLANE):
        for line in range(lines):
            lq[p, :, pl.ds(line * cb, cb)] = lg[half(core), pl.ds((line * PLANE + p) * cb, cb)]
    pl.semaphore_wait(barrier, 2 * len(mates) + len(others) + 1)

    def own_up(k):
        here = bb[k].at[block(z)]
        send(here, here, ou_s.at[k], ou_r.at[k], up)

    def own_down(k):
        here = bb[k].at[block(z)]
        send(here, here, od_s.at[k], od_r.at[k], down)

    def low(at):
        return 2 * at < lines

    for at in range(lines):

        @pl.when(z == at)
        def _():
            for k in range(chunks):
                if at < last and (at == 0 or k < (LEAD if low(at) else NEAR_LEAD)):
                    own_up(k)
                if at > 0 and (at == last or k < (NEAR_LEAD if low(at) else LEAD)):
                    own_down(k)

    for p in mates:
        send(lq.at[p], ab.at[q, half(core)], a_s, a_r.at[q], mate(p))

    def from_below(k, at):
        arrived(bb[k].at[pl.ds((at - 1) * cb, cb)], ou_r.at[k])
        if at > 1:
            arrived(bb[k].at[pl.ds(0, (at - 1) * cb)], fu_r.at[k])

    def from_above(k, at):
        arrived(bb[k].at[pl.ds((at + 1) * cb, cb)], od_r.at[k])
        if at < last - 1:
            arrived(bb[k].at[pl.ds((at + 2) * cb, (last - 1 - at) * cb)], fd_r.at[k])

    def upward(k, at):
        from_below(k, at)
        here = bb[k].at[pl.ds(0, at * cb)]
        send(here, here, fu_s.at[k], fu_r.at[k], up)

    def downward(k, at):
        from_above(k, at)
        here = bb[k].at[pl.ds((at + 1) * cb, (last - at) * cb)]
        send(here, here, fd_s.at[k], fd_r.at[k], down)

    def forward_far(k):
        for at in range(1, last):

            @pl.when(z == at)
            def _():
                (upward if low(at) else downward)(k, at)
                if k + LEAD < chunks:
                    (own_up if low(at) else own_down)(k + LEAD)

    def forward_near(k):
        for at in range(1, last):

            @pl.when(z == at)
            def _():
                (downward if low(at) else upward)(k, at)
                if k + NEAR_LEAD < chunks:
                    (own_down if low(at) else own_up)(k + NEAR_LEAD)

    def gathered(k):
        @pl.when(z == 0)
        def _():
            from_above(k, 0)

        @pl.when(z == last)
        def _():
            from_below(k, last)

    for at, (src, dst) in enumerate(small):
        pltpu.make_async_copy(src, dst, loc.at[2 * slides + 1 + at]).wait()
    weights = prior_ref[...].astype(F32) / fixed_point

    @pl.loop(0, rows // STEP_ROWS)
    def _(step):
        at = pl.ds(pl.multiple_of(step * STEP_ROWS, STEP_ROWS), STEP_ROWS)
        value = lg[at, :]
        peak = jnp.max(value, axis=1, keepdims=True)
        raised = jnp.exp(value - peak)
        scale = 1.0 / jnp.sum(raised, axis=1, keepdims=True)
        probs = raised * scale
        mass_rows = jnp.sum(probs * weights, axis=1, keepdims=True)
        rowv[0, at, :] = jnp.broadcast_to(mass_rows, (STEP_ROWS, LANES))
        rowv[1, at, :] = jnp.broadcast_to(peak, (STEP_ROWS, LANES))
        rowv[2, at, :] = jnp.broadcast_to(scale, (STEP_ROWS, LANES))
        for p in range(PLANE):
            for line in range(lines):
                at_cells = (line * PLANE + p) * cb
                pq[p, at, pl.ds(line * cb, cb)] = probs[:, at_cells : at_cells + cb]

    wide = lax.broadcasted_iota(jnp.int32, (rows, LANES), 1)
    rs[q] = jnp.where(wide == 0, rowv[1], rowv[2]).T[0:8]
    for p in mates:
        send(rs.at[q], rs.at[q], r_s, r_r.at[q], mate(p))

    rid = lax.broadcasted_iota(jnp.int32, (rows, 1), 0)
    first = rid < slide_rows
    position = place * slide_rows + jnp.where(first, rid, rid - slide_rows)
    count = jnp.where(first, count_ref[0], count_ref[1])
    valid = (position < count).astype(F32)
    scale_count = count.astype(F32)
    square = (slide_rows, slide_rows)
    eye = lax.broadcasted_iota(jnp.int32, square, 0) == lax.broadcasted_iota(jnp.int32, square, 1)
    counted = jnp.concatenate(
        [
            jnp.sum(jnp.where(eye, cells_ref[m : m + 1, :].astype(F32), 0.0), axis=1, keepdims=True)
            for m in range(slides)
        ],
        axis=0,
    )
    mass = rowv[0, :, 0:1]
    kcell = valid * counted

    def by_slide(value):
        return [jnp.sum(value[m * slide_rows : (m + 1) * slide_rows], axis=0, keepdims=True) for m in range(slides)]

    mass_parts = by_slide(valid * mass)
    cell_parts = by_slide(kcell)
    lane = lax.broadcasted_iota(jnp.int32, (1, LANES), 1)
    scalars = jnp.zeros((1, LANES), F32)
    for at, value in enumerate(mass_parts + cell_parts):
        scalars = jnp.where(lane == at, value, scalars)
    for m in range(slides):
        pltpu.make_async_copy(spatial_ref.at[m], tg.at[half(m)], loc.at[slides + m]).wait()

    head = backward_widths[0]
    t0[q] = tg[:, 0:head]
    for p in mates:
        send(t0.at[q], t0.at[q], t0_s, t0_r.at[q], mate(p))
    sacc[...] = jnp.zeros_like(sacc)
    s1[q, 3 * slides :, :] = jnp.zeros((8 - 3 * slides, genes), F32)
    s1[q, 3 * slides : 3 * slides + 1, 0:LANES] = scalars

    def share_logits():
        for p in (mates[1], mates[2], mates[0]):
            here = ab.at[p, half(core)]
            arrived(here, a_r.at[p])
            send(here, here, a2_s, a2_r.at[p], sibling)

    def lay_probs(p, at, value):
        af[p, at, :] = value
        there = pl.ds(pl.multiple_of(p * rows + at.start, BLOCK), BLOCK)
        probs_3[there, :] = threefold(value)

    def take_probs():
        in_blocks(0, rows, lambda at: lay_probs(q, at, pq[q, at, :]))
        for p in (mates[1], mates[2], mates[0]):
            arrived(rs.at[p], r_r.at[p])
            arrived(ab.at[p, half(1 - core)], a2_r.at[p])
            rowv[1] = jnp.concatenate([rs[p].T, jnp.zeros((rows, LANES - 8), F32)], axis=1)

            def take(at):
                probs = jnp.exp(ab[p, at, :] - rowv[1, at, 0:1]) * rowv[1, at, 1:2]
                lay_probs(p, at, probs)

            in_blocks(0, rows, take)

    def transpose(part):
        @pl.loop(0, PLANE // 2)
        def _(step):
            p = part * (PLANE // 2) + step
            high, low_part = halves(af[p].T)
            for third, value in enumerate((high, high, low_part)):
                turned_3[:, pl.ds(pl.multiple_of(third * PLANE * rows + p * rows, rows), rows)] = value

    def in_blocks(start, count, body):
        @pl.loop(0, count // BLOCK)
        def _(step):
            body(pl.ds(pl.multiple_of(start + step * BLOCK, BLOCK), BLOCK))

    quarter = lines * cb

    def lay_factor(at, length, width, value):
        high, low_part = halves(value)
        for third, part in enumerate((high, low_part, high)):
            here = pl.ds(pl.multiple_of(third * length + at.start, BLOCK), BLOCK)
            factor[here, 0:width] = part

    def keep_expr(k, at, value):
        start = sum(forward_widths[:k])
        for turn in range(turns):
            origin, width = sum(backward_widths[:turn]), backward_widths[turn]
            lo, hi = max(start, origin), min(start + forward_widths[k], origin + width)
            if lo < hi:
                high, low_part = halves(value[:, lo - start : hi - start])
                for third, part in enumerate((high, low_part, high)):
                    expr_3[at, pl.ds(3 * origin + third * width + lo - origin, hi - lo)] = part

    def three_turn_cols(k):
        return pl.ds(3 * sum(backward_widths[:k]), 3 * backward_widths[k])

    def forward_product(k):
        width = forward_widths[k]

        def lay(at):
            value = bb[k][at, :]
            lay_factor(at, quarter, width, value)
            keep_expr(k, at, value)

        in_blocks(0, quarter, lay)
        if k < chunks - 1:

            @pl.loop(0, PLANE * rows // TALL)
            def _(step):
                tall = pl.ds(pl.multiple_of(step * TALL, TALL), TALL)
                cs[k][tall, :] = product(probs_3[tall, :], factor[0 : 3 * quarter, 0:width], ((1,), (0,)))

            for p in mates:
                pass_pred(k, p)
        else:
            for side, served in ((1 - row, (mates[0], mates[2])), (row, (mates[1],))):
                pair = pl.ds(pl.multiple_of(2 * side * rows, 2 * rows), 2 * rows)
                cs[k][pair, :] = product(probs_3[pair, :], factor[0 : 3 * quarter, 0:width], ((1,), (0,)))
                for p in served:
                    pass_pred(k, p)

    def pass_pred(k, p):
        send(cs[k].at[share(p)], cr[k].at[q], c_s.at[k], c_r.at[k, q], mate(p))

    def finish_pred(k):
        total = cs[k][share(q), :]
        for p in mates:
            arrived(cr[k].at[p], c_r.at[k, p])
            total = total + cr[k][p]
        pr[:, cols(k)] = total
        if k == 0:
            p0[q] = total[:, 0:head]
            for p in mates:
                send(p0.at[q], p0.at[q], p0_s, p0_r.at[q], mate(p))
        truth = tg[:, cols(k)]
        for at, value in enumerate((total * truth, total * total, truth * truth)):
            sacc[at] += lane_groups(value)
        kept = valid * total
        stats = by_slide(kept * truth) + by_slide(kept * total) + by_slide(valid * truth * truth)
        s1[q, 0 : 3 * slides, cols(k)] = jnp.concatenate(stats, axis=0)

    early = sum(forward_widths[:EARLY])
    parts = (pl.ds(0, early), pl.ds(early, genes - early))

    def sum_plane(at):
        for p in mates:
            send(s1.at[q, :, parts[at]], s1.at[q, :, parts[at]], s1_s, s1_r.at[at, q], mate(p))

    def sum_line(at):
        for p in mates:
            arrived(s1.at[p, :, parts[at]], s1_r.at[at, p])
        s2[z, :, parts[at]] = (s1[0, :, parts[at]] + s1[1, :, parts[at]]) + (s1[2, :, parts[at]] + s1[3, :, parts[at]])
        for o in others:
            send(s2.at[z, :, parts[at]], s2.at[z, :, parts[at]], s2_s, s2_r.at[at, z], (o * PLANE + q, core))

    kept = {}

    def finish_genes(at):
        for o in others:
            arrived(s2.at[o, :, parts[at]], s2_r.at[at, o])
        total = s2[0, :, parts[at]]
        for line in range(1, lines):
            total = total + s2[line, :, parts[at]]
        gene_dot, gene_pred, gene_true = total[0:2], total[2:4], total[4:6]
        gene_inv = lax.rsqrt(gene_pred * gene_true + tiny)
        cos_gene = gene_dot * gene_inv
        gv[0:2, parts[at]] = gene_inv
        gv[2:4, parts[at]] = cos_gene * gene_true / (gene_pred * gene_true + tiny)
        kept["genes", at] = jnp.sum(jnp.sum(cos_gene, axis=1, keepdims=True), axis=0, keepdims=True)
        if at == 0:
            kept["mass"] = jnp.where(first, total[6:7, 0:1], total[6:7, 1:2])
            kept["cells"] = jnp.where(first, total[6:7, 2:3], total[6:7, 3:4])

    def sum_cores():
        sums = [jnp.sum(sacc[at], axis=1, keepdims=True) for at in range(3)]
        ss[q, core] = jnp.where(wide == 0, sums[0], jnp.where(wide == 1, sums[1], sums[2])).T[0:8]
        here = ss.at[q, core]
        send(here, here, ss_s.at[0], ss_r.at[q, core], sibling)
        for p in mates:
            send(here, here, ss_s.at[1], ss_r.at[q, core], mate(p))
            send(here, here, ss_s.at[1], ss_r.at[q, core], across(p))
        sacc[0] = jnp.zeros_like(sacc[0])

    def finish_spots():
        arrived(ss.at[q, 1 - core], ss_r.at[q, 1 - core])
        for p in mates:
            for side in range(2):
                arrived(ss.at[p, side], ss_r.at[p, side])
        lane_id = lax.broadcasted_iota(jnp.int32, (1, rows), 1)
        first_lane = lane_id < slide_rows
        lane_spot = jnp.where(first_lane, lane_id, lane_id - slide_rows)
        lane_count = jnp.where(first_lane, count_ref[0], count_ref[1])
        for p in range(PLANE):
            lane_valid = ((z * PLANE + p) * slide_rows + lane_spot < lane_count).astype(F32)
            spot = ss[p, 0] + ss[p, 1]
            spot_dot, spot_pred, spot_true = spot[0:1], spot[1:2], spot[2:3]
            spot_inv = lax.rsqrt(spot_pred * spot_true + tiny)
            cos_spot = spot_dot * spot_inv
            spot_back = cos_spot * spot_true / (spot_pred * spot_true + tiny)
            vectors = [lane_valid * spot_inv, lane_valid * spot_back, lane_valid, lane_valid * cos_spot]
            vr[p] = jnp.concatenate(vectors + [jnp.zeros((4, rows), F32)], axis=0)
        kept["cos"] = jnp.sum(vr[q, 3:4, :], axis=1, keepdims=True)

    def gradient(truth, guess, by_row, k):
        pieces = []
        for m in range(slides):
            lo, hi = m * slide_rows, (m + 1) * slide_rows
            inverse, back = gv[m : m + 1, turn_cols(k)], gv[2 + m : 3 + m, turn_cols(k)]
            spot_inv, spot_back, spot_valid = by_row[lo:hi, 0:1], by_row[lo:hi, 1:2], by_row[lo:hi, 2:3]
            pieces.append(
                guess[lo:hi] * (spot_valid * back + spot_back) - truth[lo:hi] * (spot_valid * inverse + spot_inv)
            )
        return jnp.concatenate(pieces, axis=0)

    def head_gradient():
        for p in mates:
            arrived(t0.at[p], t0_r.at[p])
            arrived(p0.at[p], p0_r.at[p])
        for p in range(PLANE):
            ds[0][share(p), :] = gradient(t0[p], p0[p], vr[p].T, 0)
        sacc[0] += lane_groups(ds[0][share(q), :] * p0[q])

    def send_grad(k):
        if k == 0:
            kept["by_row"] = vr[q].T
            return
        grad = gradient(tg[:, turn_cols(k)], pr[:, turn_cols(k)], kept["by_row"], k)
        here = ds[k].at[share(q)]
        here[...] = grad
        for p in mates:
            send(here, here, d_s.at[k], d_r.at[k, q], mate(p))
        sacc[0] += lane_groups(grad * pr[:, turn_cols(k)])

    def send_terms():
        mass_total, cell_total = kept["mass"], kept["cells"]
        portion = kcell / cell_total
        kl_rows = portion * (jnp.log(counted) - jnp.log(cell_total) - jnp.log(mass) + jnp.log(mass_total))
        dmass = scale_count * valid * (1.0 / mass_total - portion / mass)
        terms = jnp.sum(scale_count * kl_rows, axis=0, keepdims=True) - kept["cos"]
        l1[q] = jnp.broadcast_to(terms, (8, LANES))
        for p in mates:
            send(l1.at[q], l1.at[q], l1_s, l1_r.at[q], mate(p))
        inner = jnp.sum(sacc[0], axis=1, keepdims=True)
        inn[core] = jnp.where(wide == 0, inner, kept["genes", 0] + kept["genes", 1])
        send(inn.at[core], inn.at[core], in_s, in_r, sibling)
        rowv[1] = jnp.broadcast_to(dmass, (rows, LANES))

    middle = lines // 2

    def backward_product(k):
        if k == 0:
            head_gradient()
        else:
            for p in mates:
                arrived(ds[k].at[share(p)], d_r.at[k, p])
        width, spots = backward_widths[k], PLANE * rows

        def lay(at):
            value = ds[k][at, :]
            lay_factor(at, spots, width, value)
            grad_3[at, three_turn_cols(k)] = threefold(value)

        in_blocks(0, spots, lay)
        if not halved(k):

            @pl.loop(0, quarter // TALL)
            def _(step):
                tall = pl.ds(pl.multiple_of(step * TALL, TALL), TALL)
                es[k][tall, :] = product(turned_3[tall, :], factor[0 : 3 * spots, 0:width], ((1,), (0,)))

        for turn in range(2):
            if halved(k):
                side = (1 - z // middle) if turn == 0 else z // middle
                pair = pl.ds(pl.multiple_of(side * middle * cb, middle * cb), middle * cb)
                es[k][pair, :] = product(turned_3[pair, :], factor[0 : 3 * spots, 0:width], ((1,), (0,)))

            @pl.when(z == 0)
            def _():
                if halved(k):
                    pass_up(k, middle if turn == 0 else 1, middle if turn == 0 else middle - 1, turn)
                elif whole(k):
                    if turn == 0:
                        pass_up(k, 1, last, 0)
                elif turn == 0:
                    for line in range(last, 0, -1):
                        pass_up(k, line, 1, line)

            @pl.when(z == last)
            def _():
                if halved(k):
                    pass_down(k, 0 if turn == 0 else middle, middle if turn == 0 else middle - 1, turn)
                elif whole(k):
                    if turn == 0:
                        pass_down(k, 0, last, 0)
                elif turn == 0:
                    for line in range(last):
                        pass_down(k, line, 1, line)

    def halved(k):
        return k == 0

    def whole(k):
        return 0 < k < turns - SPLIT

    def pass_up(k, line, count, slot):
        here = pl.ds(line * cb, count * cb)
        send(es[k].at[here], ru[k].at[here], ru_s.at[k], ru_r.at[k, slot], up)

    def pass_down(k, line, count, slot):
        here = pl.ds(line * cb, count * cb)
        send(es[k].at[here], rd[k].at[here], rd_s.at[k], rd_r.at[k, slot], down)

    def take_up(k, line, count, slot):
        arrived(ru[k].at[pl.ds(line * cb, count * cb)], ru_r.at[k, slot])

    def take_down(k, line, count, slot):
        arrived(rd[k].at[pl.ds(line * cb, count * cb)], rd_r.at[k, slot])

    def add_up(k, line, count):
        def add(at):
            es[k][at, :] += ru[k][at, :]

        in_blocks(line * cb, count * cb, add)

    def add_down(k, line, count):
        def add(at):
            es[k][at, :] += rd[k][at, :]

        in_blocks(line * cb, count * cb, add)

    def rising(k, at):
        if halved(k) or whole(k):
            start = middle if halved(k) else at
            take_up(k, start, lines - start, 0)
            above = max(at + 1, start)
            add_up(k, above, lines - above)
            pass_up(k, above, lines - above, 0)
        else:
            for line in range(last, at, -1):
                take_up(k, line, 1, line)
                add_up(k, line, 1)
                pass_up(k, line, 1, line)

    def falling(k, at):
        if halved(k) or whole(k):
            end = middle if halved(k) else at + 1
            take_down(k, 0, end, 0)
            below = min(at, end)
            add_down(k, 0, below)
            pass_down(k, 0, below, 0)
        else:
            for line in range(at):
                take_down(k, line, 1, line)
                add_down(k, line, 1)
                pass_down(k, line, 1, line)

    def add_near(k):
        for at in range(1, last):

            @pl.when(z == at)
            def _():
                (rising if low(at) else falling)(k, at)

    def add_far(k):
        for at in range(1, last):

            @pl.when(z == at)
            def _():
                (falling if low(at) else rising)(k, at)

    def finish_expr(k):
        for at in range(lines):

            @pl.when(z == at)
            def _():
                if at > 0:
                    if halved(k) and at < middle:
                        take_up(k, at, 1, 1)
                    elif at == last and (halved(k) or whole(k)):
                        take_up(k, at, 1, 0)
                    elif not halved(k) and not whole(k):
                        take_up(k, at, 1, at)
                if at < last:
                    if halved(k) and at >= middle:
                        take_down(k, at, 1, 1)
                    elif at == 0 and (halved(k) or whole(k)):
                        take_down(k, at, 1, 0)
                    elif not halved(k) and not whole(k):
                        take_down(k, at, 1, at)

        from_low, from_high = z > 0, z < last

        @pl.loop(0, cb // BLOCK)
        def _(step):
            here = pl.ds(pl.multiple_of(step * BLOCK, BLOCK), BLOCK)
            own = pl.ds(pl.multiple_of(z * cb + step * BLOCK, BLOCK), BLOCK)
            total = es[k][own, :]
            total = total + jnp.where(from_low, ru[k][own, :], 0.0)
            ge[here, turn_cols(k)] = total + jnp.where(from_high, rd[k][own, :], 0.0)

    def probs_gradient(k):
        at = three_turn_cols(k)
        if k == turns - 1:
            return

        @pl.loop(0, PLANE * rows // TALL)
        def _(step):
            tall = pl.ds(pl.multiple_of(step * TALL, TALL), TALL)
            part = product(grad_3[tall, at], expr_3[:, at], ((1,), (1,)))
            if k == 0:
                fs[tall, :] = part
            else:
                fs[tall, :] += part

    def slide_of(p, m):
        return pl.ds(pl.multiple_of(p * rows + m * slide_rows, slide_rows), slide_rows)

    def sum_probs_cores():
        at = three_turn_cols(turns - 1)
        for p in mates + (q,):
            fs[share(p), :] += product(grad_3[share(p), at], expr_3[:, at], ((1,), (1,)))
            fx[p] = fs[slide_of(p, 1 - core), :]
            send(fx.at[p], fy.at[p], fx_s, fx_r.at[p], sibling)

    def return_probs():
        for p in mates:
            arrived(fy.at[p], fx_r.at[p])
            fz[p] = fs[slide_of(p, core), :] + fy[p]
            send(fz.at[p], fr.at[q], f_s, f_r.at[q], mate(p))
        arrived(fy.at[q], fx_r.at[q])
        fr[q] = fs[slide_of(q, core), :] + fy[q]

    def pass_terms():
        for p in mates:
            arrived(l1.at[p], l1_r.at[p])
        l2[z] = (l1[0] + l1[1]) + (l1[2] + l1[3])
        for o in others:
            send(l2.at[z], l2.at[z], l2_s, l2_r.at[z], (o * PLANE + q, core))

    def part_of(slide, m):
        start = slide * slide_rows + m * (slide_rows // 2)
        return pl.ds(pl.multiple_of(start, slide_rows // 2), slide_rows // 2)

    def finish_logits():
        arrived(inn.at[1 - core], in_r)
        rowv[2] = (inn[0] + inn[1]) + rowv[1] * rowv[0]
        for p in mates:
            arrived(fr.at[p], f_r.at[p])
        for m in range(2):

            @pl.loop(0, slide_rows // STEP_ROWS // 2)
            def _(step):
                row_at = (m * (slide_rows // STEP_ROWS // 2) + step) * STEP_ROWS
                at = pl.ds(pl.multiple_of(row_at, STEP_ROWS), STEP_ROWS)
                whole_at = pl.ds(pl.multiple_of(core * slide_rows + row_at, STEP_ROWS), STEP_ROWS)
                by_mass, total_inner = rowv[1, whole_at, 0:1], rowv[2, whole_at, 0:1]
                for p in range(PLANE):
                    for line in range(lines):
                        here, there = pl.ds(line * cb, cb), (line * PLANE + p) * cb
                        grad = fr[p, at, here] + by_mass * weights[:, there : there + cb]
                        glog[whole_at, pl.ds(there, cb)] = pq[p, whole_at, here] * (grad - total_inner)

            here = part_of(core, m)
            send(glog.at[here], glog.at[here], go_s, go_r.at[m], sibling)

    def forward_left():
        for k in range(chunks):

            @pl.when(z < last)
            def _():
                sent(bb[k].at[block(z)], ou_s.at[k])

            @pl.when(z > 0)
            def _():
                sent(bb[k].at[block(z)], od_s.at[k])

            for at in range(1, last):

                @pl.when(z == at)
                def _():
                    sent(bb[k].at[pl.ds(0, at * cb)], fu_s.at[k])
                    sent(bb[k].at[pl.ds((at + 1) * cb, (last - at) * cb)], fd_s.at[k])

        three = pl.ds(0, len(mates))
        sent(ab.at[three, half(0)], a_s)
        sent(ab.at[three, half(0)], a2_s)
        sent(rs.at[three], r_s)
        sent(t0.at[three], t0_s)
        sent(p0.at[three], p0_s)
        for k in range(chunks):
            sent(cr[k].at[three], c_s.at[k])
        sent(s1.at[three], s1_s)
        sent(s2.at[pl.ds(0, last)], s2_s)
        sent(ss.at[0, 0], ss_s.at[0])
        sent(ss.at[three], ss_s.at[1])

    steps = {
        "far": forward_far,
        "near": forward_near,
        "share": share_logits,
        "take": take_probs,
        "whole": gathered,
        "product": forward_product,
        "sum": finish_pred,
        "turn": transpose,
        "plane": sum_plane,
        "line": sum_line,
        "genes": finish_genes,
        "cores": sum_cores,
        "spots": finish_spots,
        "grad": send_grad,
        "terms": send_terms,
        "backward": backward_product,
        "probs": probs_gradient,
        "exchange": sum_probs_cores,
        "return": return_probs,
        "loss": pass_terms,
        "logits": finish_logits,
        "add_near": add_near,
        "add_far": add_far,
        "expr": finish_expr,
        "left": forward_left,
    }
    for name, *where in STEPS:
        steps[name](*where)

    for o in others:
        arrived(l2.at[o], l2_r.at[o])
    loss = l2[0]
    for line in range(1, lines):
        loss = loss + l2[line]
    loss_ref[...] = loss[0:1, 0:1] - (inn[0, 0:1, 1:2] + inn[1, 0:1, 1:2])
    for m in range(2):
        arrived(glog.at[part_of(1 - core, m)], go_r.at[m])

    for k in range(turns):
        for at in range(lines):

            @pl.when(z == at)
            def _():
                if at < last:
                    sent(es[k].at[pl.ds((at + 1) * cb, (last - at) * cb)], ru_s.at[k])
                if at > 0:
                    sent(es[k].at[pl.ds(0, at * cb)], rd_s.at[k])

    three = pl.ds(0, len(mates))
    for k in range(1, turns):
        sent(ds[k].at[pl.ds(0, len(mates) * rows)], d_s.at[k])
    sent(inn.at[0], in_s)
    sent(l1.at[three], l1_s)
    sent(l2.at[pl.ds(0, last)], l2_s)
    sent(fr.at[three], f_s)
    sent(fx, fx_s)
    sent(glog.at[half(0)], go_s)


def lane_groups(value):
    parts = [value[:, at : at + LANES] for at in range(0, value.shape[1], LANES)]
    return functools.reduce(lambda a, b: a + b, parts)


def grouped(refs, sizes):
    at = 0
    for size in sizes:
        yield refs[at : at + size]
        at += size


def deliver(pred_in, loss_in, glog_in, gexp_in, pred_ref, loss_ref, glog_ref, gexp_ref, sems):
    slides, slide_rows = pred_ref.shape[0], pred_ref.shape[1]
    pairs = [(gexp_in, gexp_ref), (loss_in, loss_ref)]
    for m in range(slides):
        part = pl.ds(m * slide_rows, slide_rows)
        pairs += [(glog_in.at[part], glog_ref.at[m]), (pred_in.at[part], pred_ref.at[m])]
    copies = [pltpu.make_async_copy(src, dst, sems.at[at]) for at, (src, dst) in enumerate(pairs)]
    for copy in copies:
        copy.start()
    for copy in copies:
        copy.wait()


def plane_call(logits, expr, spatial, slide_spots, spot_cells, cell_prior, lines):
    slides, slide_rows, cells = logits.shape
    rows = slides * slide_rows
    cb, genes = expr.shape
    quarter = lines * cb
    spots = PLANE * rows
    chunks, turns = len(FORWARD), len(BACKWARD)
    dma = pltpu.SemaphoreType.DMA
    vmem = pltpu.VMEM
    anywhere = pl.BlockSpec(memory_space=pl.ANY)
    in_vmem = pl.BlockSpec(memory_space=pltpu.VMEM)
    scratch = [
        pltpu.SMEM((slides,), jnp.int32),
        vmem((slides, slide_rows), jnp.int32),
        vmem((1, cells), jnp.int32),
        vmem((rows, cells), F32),
        vmem((PLANE, slide_rows, quarter), F32),
        vmem((rows, genes), F32),
        vmem((cb, genes), F32),
        vmem((PLANE, rows, quarter), F32),
        vmem((PLANE, rows, quarter), F32),
        vmem((PLANE, rows, quarter), F32),
        vmem((spots, 3 * quarter), BF16),
        vmem((quarter, 3 * spots), BF16),
        vmem((quarter, 3 * genes), BF16),
        vmem((3, rows, LANES), F32),
        vmem((PLANE, 8, genes), F32),
        vmem((lines, 8, genes), F32),
        vmem((8, genes), F32),
        vmem((PLANE, 2, 8, rows), F32),
        vmem((3, rows, LANES), F32),
        vmem((PLANE, 8, rows), F32),
        vmem((spots, 3 * genes), BF16),
        vmem((3 * max(quarter, spots), max(FORWARD + BACKWARD)), BF16),
        vmem((PLANE, rows, BACKWARD[0]), F32),
        vmem((PLANE, rows, BACKWARD[0]), F32),
        vmem((PLANE, 8, rows), F32),
        vmem((spots, quarter), F32),
        vmem((PLANE, slide_rows, quarter), F32),
        vmem((PLANE, slide_rows, quarter), F32),
        vmem((PLANE, slide_rows, quarter), F32),
        vmem((PLANE, slide_rows, quarter), F32),
        vmem((2, rows, LANES), F32),
        vmem((PLANE, 8, LANES), F32),
        vmem((lines, 8, LANES), F32),
        dma((2 * slides + 4,)),
        dma((chunks,)),
        dma((chunks,)),
        dma((chunks,)),
        dma((chunks,)),
        dma((chunks,)),
        dma((chunks,)),
        dma((chunks,)),
        dma((chunks,)),
        dma,
        dma((PLANE,)),
        dma,
        dma((PLANE,)),
        dma,
        dma((PLANE,)),
        dma((chunks,)),
        dma((chunks, PLANE)),
        dma,
        dma((2, PLANE)),
        dma,
        dma((2, lines)),
        dma((2,)),
        dma((PLANE, 2)),
        dma((turns,)),
        dma((turns, PLANE)),
        dma((turns,)),
        dma((turns, lines)),
        dma((turns,)),
        dma((turns, lines)),
        dma,
        dma((PLANE,)),
        dma,
        dma((PLANE,)),
        dma,
        dma((2,)),
        dma,
        dma,
        dma,
        dma((PLANE,)),
        dma,
        dma((lines,)),
        dma,
        dma((PLANE,)),
        dma,
        dma((PLANE,)),
    ]
    for shape, widths in (
        ((quarter,), FORWARD),
        ((spots,), FORWARD),
        ((PLANE, rows), FORWARD),
        ((spots,), BACKWARD),
        ((quarter,), BACKWARD),
        ((quarter,), BACKWARD),
        ((quarter,), BACKWARD),
    ):
        scratch += [vmem(shape + (width,), F32) for width in widths]
    in_hbm = functools.partial(pltpu.with_memory_space_constraint, memory_space=pltpu.HBM)
    in_place = functools.partial(pltpu.with_memory_space_constraint, memory_space=pltpu.VMEM)
    results = pl.pallas_call(
        functools.partial(plane_kernel, lines, FORWARD, BACKWARD),
        out_shape=(
            vmem((rows, genes), F32),
            vmem((1, 1), F32),
            vmem((rows, cells), F32),
            vmem((cb, genes), F32),
        ),
        in_specs=[anywhere] * 6,
        out_specs=(in_vmem,) * 4,
        scratch_shapes=scratch,
        compiler_params=pltpu.CompilerParams(
            collective_id=0, has_side_effects=True, vmem_limit_bytes=48 * 1024 * 1024
        ),
    )(*map(in_hbm, (logits, expr, spatial, slide_spots, spot_cells, cell_prior.reshape(1, cells))))
    pred, loss, grad_logits, grad_expr = pl.pallas_call(
        deliver,
        out_shape=(
            jax.ShapeDtypeStruct((slides, slide_rows, genes), F32),
            jax.ShapeDtypeStruct((1, 1), F32),
            jax.ShapeDtypeStruct((slides, slide_rows, cells), F32),
            jax.ShapeDtypeStruct((cb, genes), F32),
        ),
        in_specs=[anywhere] * 4,
        out_specs=(anywhere,) * 4,
        scratch_shapes=[dma((2 * slides + 2,))],
        compiler_params=pltpu.CompilerParams(vmem_limit_bytes=4 * 1024 * 1024),
    )(*map(in_place, results))
    return pred, loss.reshape(()), grad_logits, grad_expr


def general_plan(logits, expr, spatial, slide_spots, spot_cells, cell_prior):
    place = lax.axis_index("spot")
    side = lax.axis_index("gene")
    rows_all = logits.shape[1]
    cell_rows = expr.shape[0]
    weights = cell_prior.astype(jnp.float32) / fixed_point
    gene_share = (place == 0).astype(jnp.float32)
    row_share = (side == 0).astype(jnp.float32)
    own_weights = lax.dynamic_slice_in_dim(weights, place * cell_rows, cell_rows, 0)
    expr_acc = jnp.zeros((cell_rows, expr.shape[1]), jnp.float32)
    loss_local = jnp.zeros((), jnp.float32)
    pred_list = []
    grad_list = []
    for slide in range(logits.shape[0]):
        logit_rows = logits[slide]
        counted = spot_cells[slide].astype(jnp.float32)
        target = spatial[slide]
        positions = place * rows_all + jnp.arange(rows_all, dtype=jnp.int32)
        valid = (positions < slide_spots[slide]).astype(jnp.float32)
        peak = jnp.max(logit_rows, axis=1, keepdims=True)
        raised = jnp.exp(logit_rows - peak)
        probs = raised / jnp.sum(raised, axis=1, keepdims=True)
        mass = jnp.dot(probs, weights, precision=lax.Precision.HIGHEST)
        blocks = lax.all_to_all(probs, "spot", split_axis=1, concat_axis=0, tiled=True)
        pred = lax.psum_scatter(
            jnp.dot(blocks, expr, precision=lax.Precision.HIGHEST),
            "spot",
            scatter_dimension=0,
            tiled=True,
        )
        gene_dot = jnp.sum(valid[:, None] * pred * target, axis=0)
        gene_pred = jnp.sum(valid[:, None] * pred * pred, axis=0)
        gene_true = jnp.sum(valid[:, None] * target * target, axis=0)
        mass_part = jnp.sum(valid * mass)
        kcell = valid * counted
        cell_part = jnp.sum(kcell)
        spot_dot = jnp.sum(pred * target, axis=1)
        spot_pred = jnp.sum(pred * pred, axis=1)
        spot_true = jnp.sum(target * target, axis=1)
        gene_dot, gene_pred, gene_true, mass_total, cell_total = lax.psum(
            (gene_dot, gene_pred, gene_true, mass_part, cell_part), "spot"
        )
        spot_dot, spot_pred, spot_true = lax.psum((spot_dot, spot_pred, spot_true), "gene")
        gene_inv = lax.rsqrt(gene_pred * gene_true + tiny)
        cos_gene = gene_dot * gene_inv
        spot_inv = lax.rsqrt(spot_pred * spot_true + tiny)
        cos_spot = spot_dot * spot_inv
        share = kcell / cell_total
        scale_count = slide_spots[slide].astype(jnp.float32)
        kl_part = jnp.sum(
            share * (jnp.log(counted) - jnp.log(cell_total) - jnp.log(mass) + jnp.log(mass_total))
        )
        loss_local = loss_local - gene_share * jnp.sum(cos_gene)
        loss_local = loss_local + row_share * (scale_count * kl_part - jnp.sum(valid * cos_spot))
        gene_back = cos_gene * gene_true / (gene_pred * gene_true + tiny)
        spot_back = cos_spot * spot_true / (spot_pred * spot_true + tiny)
        dpred = -valid[:, None] * (
            target * (gene_inv[None, :] + spot_inv[:, None])
            - pred * gene_back[None, :]
            - pred * spot_back[:, None]
        )
        dmass = scale_count * valid * (1.0 / mass_total - share / mass)
        pred_list.append(pred)
        grads_full, mass_full = (
            lax.all_gather(dpred, "spot", axis=0, tiled=True),
            lax.all_gather(dmass, "spot", axis=0, tiled=True),
        )
        dprob_cells = jnp.dot(grads_full, expr.T, precision=lax.Precision.HIGHEST)
        dprob_cells = lax.psum(dprob_cells, "gene")
        expr_acc = expr_acc + lax.dot_general(
            blocks, grads_full, (((0,), (0,)), ((), ())), precision=lax.Precision.HIGHEST
        )
        dprob_cells = dprob_cells + mass_full[:, None] * own_weights[None, :]
        dprob_rows = lax.all_to_all(dprob_cells, "spot", split_axis=0, concat_axis=1, tiled=True)
        inner = jnp.sum(probs * dprob_rows, axis=1, keepdims=True)
        dlogit = probs * (dprob_rows - inner)
        grad_list.append(dlogit)
    loss = lax.psum(loss_local, ("spot", "gene"))
    return (jnp.stack(pred_list), loss, jnp.stack(grad_list), expr_acc)


def solution(mesh):
    places = mesh.shape["spot"]

    def on_device(logits, expr, spatial, slide_spots, spot_cells, cell_prior):
        if places == PLANE * PLANE and mesh.shape["gene"] == 2 and expr.shape[1] == sum(FORWARD):
            return plane_call(
                logits, expr, spatial, slide_spots, spot_cells, cell_prior, places // PLANE
            )
        return general_plan(logits, expr, spatial, slide_spots, spot_cells, cell_prior)

    in_specs = (
        P(None, "spot", None),
        P("spot", "gene"),
        P(None, "spot", "gene"),
        P(),
        P(None, "spot"),
        P(),
    )
    out_specs = (P(None, "spot", "gene"), P(), P(None, "spot", None), P("spot", "gene"))
    return jax.shard_map(
        on_device, mesh=mesh, in_specs=in_specs, out_specs=out_specs, check_vma=False
    )
```

```python
import functools

import jax
import jax.numpy as jnp
from jax import lax
from jax.experimental import pallas as pl
from jax.experimental.pallas import tpu as pltpu
from jax.sharding import PartitionSpec as P

tiny = 1e-06
fixed_point = 16384.0
F32 = jnp.float32
BF16 = jnp.bfloat16
MESH = pl.DeviceIdType.MESH

PLANE = 4
LANES = 128
STEP_ROWS = 16
BLOCK = 32
TALL = 256
FORWARD = (128, 256, 256, 256, 128)
BACKWARD = (128, 128, 256, 256, 256)
SPLIT = 2
LEAD = 2
NEAR_LEAD = 3
EARLY = 4
STEPS = (
    ("far", 0),
    ("far", 1),
    ("near", 0),
    ("share",),
    ("far", 2),
    ("far", 3),
    ("take",),
    ("whole", 0),
    ("near", 1),
    ("product", 0),
    ("sum", 0),
    ("whole", 1),
    ("near", 2),
    ("product", 1),
    ("whole", 2),
    ("product", 2),
    ("whole", 3),
    ("near", 3),
    ("product", 3),
    ("whole", 4),
    ("far", 4),
    ("near", 4),
    ("turn", 0),
    ("sum", 1),
    ("sum", 2),
    ("product", 4),
    ("turn", 1),
    ("sum", 3),
    ("plane", 0),
    ("sum", 4),
    ("plane", 1),
    ("cores",),
    ("line", 0),
    ("spots",),
    ("genes", 0),
    ("grad", 0),
    ("grad", 1),
    ("grad", 2),
    ("line", 1),
    ("backward", 0),
    ("grad", 3),
    ("backward", 1),
    ("add_near", 0),
    ("genes", 1),
    ("backward", 2),
    ("probs", 0),
    ("add_far", 0),
    ("probs", 1),
    ("expr", 0),
    ("grad", 4),
    ("add_near", 1),
    ("probs", 2),
    ("terms",),
    ("backward", 3),
    ("probs", 3),
    ("add_near", 2),
    ("backward", 4),
    ("add_far", 1),
    ("probs", 4),
    ("exchange",),
    ("add_near", 3),
    ("add_far", 2),
    ("left",),
    ("return",),
    ("loss",),
    ("add_far", 3),
    ("expr", 1),
    ("add_near", 4),
    ("logits",),
    ("add_far", 4),
    ("expr", 2),
    ("expr", 3),
    ("expr", 4),
)


def halves(value):
    high = value.astype(BF16)
    return high, (value - high.astype(F32)).astype(BF16)


def threefold(value):
    high, low = halves(value)
    return jnp.concatenate([high, high, low], axis=1)


def product(a, b, contract):
    return lax.dot_general(a, b, (contract, ((), ())), preferred_element_type=F32)


def plane_kernel(lines, forward_widths, backward_widths, *refs):
    chunks, turns = len(forward_widths), len(backward_widths)
    (
        (logits_ref, expr_ref, spatial_ref, count_in, cells_in, prior_in),
        (pr, loss_ref, glog, ge),
        (count_ref, cells_ref, prior_ref, lg, lq, tg, ex, pq, ab, af, probs_3, turned_3, expr_3, sacc, s1, s2, gv, ss, rowv, rs),
        (grad_3, factor, t0, p0, vr, fs, fx, fy, fz, fr, inn, l1, l2),
        (loc, ou_s, ou_r, od_s, od_r, fu_s, fu_r, fd_s, fd_r, a_s, a_r, a2_s, a2_r, r_s, r_r),
        (c_s, c_r, s1_s, s1_r, s2_s, s2_r, ss_s, ss_r, d_s, d_r, ru_s, ru_r, rd_s, rd_r),
        (f_s, f_r, fx_s, fx_r, go_s, go_r, in_s, in_r, l1_s, l1_r, l2_s, l2_r, t0_s, t0_r, p0_s, p0_r),
        bb,
        cs,
        cr,
        ds,
        es,
        ru,
        rd,
    ) = grouped(refs, (6, 4, 20, 13, 15, 14, 16, chunks, chunks, chunks, turns, turns, turns, turns))
    place = lax.axis_index("spot")
    core = lax.axis_index("gene")
    z = place // PLANE
    q = place % PLANE
    col, row = q % 2, q // 2
    mates = ((1 - row) * 2 + 1 - col, row * 2 + 1 - col, (1 - row) * 2 + col)
    others = tuple((z + step) % lines for step in range(1, lines))
    up, down = (place + PLANE, core), (place - PLANE, core)
    sibling = (place, 1 - core)
    slides, slide_rows = logits_ref.shape[0], logits_ref.shape[1]
    rows = slides * slide_rows
    cb = expr_ref.shape[0]
    genes = expr_ref.shape[1]
    last = lines - 1

    def mate(p):
        return (z * PLANE + p, core)

    def across(p):
        return (z * PLANE + p, 1 - core)

    def send(src, dst, send_sem, recv_sem, device):
        copy = pltpu.make_async_remote_copy(
            src_ref=src, dst_ref=dst, send_sem=send_sem, recv_sem=recv_sem, device_id=device, device_id_type=MESH
        )
        copy.start()

    def arrived(dst, recv_sem):
        pltpu.make_async_copy(dst, dst, recv_sem).wait()

    sent = arrived

    def cols(k):
        return pl.ds(sum(forward_widths[:k]), forward_widths[k])

    def turn_cols(k):
        return pl.ds(sum(backward_widths[:k]), backward_widths[k])

    def block(index):
        return pl.ds(pl.multiple_of(index * cb, cb), cb)

    def share(index):
        return pl.ds(pl.multiple_of(index * rows, rows), rows)

    def half(index):
        return pl.ds(pl.multiple_of(index * slide_rows, slide_rows), slide_rows)

    small = ((prior_in, prior_ref), (count_in, count_ref), (cells_in, cells_ref))
    pltpu.make_async_copy(expr_ref, ex, loc.at[2 * slides]).start()
    for m in range(slides):
        pltpu.make_async_copy(logits_ref.at[m], lg.at[half(m)], loc.at[m]).start()
    for at, (src, dst) in enumerate(small):
        pltpu.make_async_copy(src, dst, loc.at[2 * slides + 1 + at]).start()
    for m in range(slides):
        pltpu.make_async_copy(spatial_ref.at[m], tg.at[half(m)], loc.at[slides + m]).start()

    barrier = pltpu.get_barrier_semaphore()
    for p in mates:
        pl.semaphore_signal(barrier, inc=1, device_id=mate(p), device_id_type=MESH)
        pl.semaphore_signal(barrier, inc=1, device_id=across(p), device_id_type=MESH)
    for o in others:
        pl.semaphore_signal(barrier, inc=1, device_id=(o * PLANE + q, core), device_id_type=MESH)
    pl.semaphore_signal(barrier, inc=1, device_id=sibling, device_id_type=MESH)
    pltpu.make_async_copy(expr_ref, ex, loc.at[2 * slides]).wait()
    for k in range(chunks):
        bb[k][block(z), :] = ex[:, cols(k)]
    for m in range(slides):
        pltpu.make_async_copy(logits_ref.at[m], lg.at[half(m)], loc.at[m]).wait()
    for p in range(PLANE):
        for line in range(lines):
            lq[p, :, pl.ds(line * cb, cb)] = lg[half(core), pl.ds((line * PLANE + p) * cb, cb)]
    pl.semaphore_wait(barrier, 2 * len(mates) + len(others) + 1)

    def own_up(k):
        here = bb[k].at[block(z)]
        send(here, here, ou_s.at[k], ou_r.at[k], up)

    def own_down(k):
        here = bb[k].at[block(z)]
        send(here, here, od_s.at[k], od_r.at[k], down)

    def low(at):
        return 2 * at < lines

    for at in range(lines):

        @pl.when(z == at)
        def _():
            for k in range(chunks):
                if at < last and (at == 0 or k < (LEAD if low(at) else NEAR_LEAD)):
                    own_up(k)
                if at > 0 and (at == last or k < (NEAR_LEAD if low(at) else LEAD)):
                    own_down(k)

    for p in mates:
        send(lq.at[p], ab.at[q, half(core)], a_s, a_r.at[q], mate(p))

    def from_below(k, at):
        arrived(bb[k].at[pl.ds((at - 1) * cb, cb)], ou_r.at[k])
        if at > 1:
            arrived(bb[k].at[pl.ds(0, (at - 1) * cb)], fu_r.at[k])

    def from_above(k, at):
        arrived(bb[k].at[pl.ds((at + 1) * cb, cb)], od_r.at[k])
        if at < last - 1:
            arrived(bb[k].at[pl.ds((at + 2) * cb, (last - 1 - at) * cb)], fd_r.at[k])

    def upward(k, at):
        from_below(k, at)
        here = bb[k].at[pl.ds(0, at * cb)]
        send(here, here, fu_s.at[k], fu_r.at[k], up)

    def downward(k, at):
        from_above(k, at)
        here = bb[k].at[pl.ds((at + 1) * cb, (last - at) * cb)]
        send(here, here, fd_s.at[k], fd_r.at[k], down)

    def forward_far(k):
        for at in range(1, last):

            @pl.when(z == at)
            def _():
                (upward if low(at) else downward)(k, at)
                if k + LEAD < chunks:
                    (own_up if low(at) else own_down)(k + LEAD)

    def forward_near(k):
        for at in range(1, last):

            @pl.when(z == at)
            def _():
                (downward if low(at) else upward)(k, at)
                if k + NEAR_LEAD < chunks:
                    (own_down if low(at) else own_up)(k + NEAR_LEAD)

    def gathered(k):
        @pl.when(z == 0)
        def _():
            from_above(k, 0)

        @pl.when(z == last)
        def _():
            from_below(k, last)

    for at, (src, dst) in enumerate(small):
        pltpu.make_async_copy(src, dst, loc.at[2 * slides + 1 + at]).wait()
    weights = prior_ref[...].astype(F32) / fixed_point

    @pl.loop(0, rows // STEP_ROWS)
    def _(step):
        at = pl.ds(pl.multiple_of(step * STEP_ROWS, STEP_ROWS), STEP_ROWS)
        value = lg[at, :]
        peak = jnp.max(value, axis=1, keepdims=True)
        raised = jnp.exp(value - peak)
        scale = 1.0 / jnp.sum(raised, axis=1, keepdims=True)
        probs = raised * scale
        mass_rows = jnp.sum(probs * weights, axis=1, keepdims=True)
        rowv[0, at, :] = jnp.broadcast_to(mass_rows, (STEP_ROWS, LANES))
        rowv[1, at, :] = jnp.broadcast_to(peak, (STEP_ROWS, LANES))
        rowv[2, at, :] = jnp.broadcast_to(scale, (STEP_ROWS, LANES))
        for p in range(PLANE):
            for line in range(lines):
                at_cells = (line * PLANE + p) * cb
                pq[p, at, pl.ds(line * cb, cb)] = probs[:, at_cells : at_cells + cb]

    wide = lax.broadcasted_iota(jnp.int32, (rows, LANES), 1)
    rs[q] = jnp.where(wide == 0, rowv[1], rowv[2]).T[0:8]
    for p in mates:
        send(rs.at[q], rs.at[q], r_s, r_r.at[q], mate(p))

    rid = lax.broadcasted_iota(jnp.int32, (rows, 1), 0)
    first = rid < slide_rows
    position = place * slide_rows + jnp.where(first, rid, rid - slide_rows)
    count = jnp.where(first, count_ref[0], count_ref[1])
    valid = (position < count).astype(F32)
    scale_count = count.astype(F32)
    square = (slide_rows, slide_rows)
    eye = lax.broadcasted_iota(jnp.int32, square, 0) == lax.broadcasted_iota(jnp.int32, square, 1)
    counted = jnp.concatenate(
        [
            jnp.sum(jnp.where(eye, cells_ref[m : m + 1, :].astype(F32), 0.0), axis=1, keepdims=True)
            for m in range(slides)
        ],
        axis=0,
    )
    mass = rowv[0, :, 0:1]
    kcell = valid * counted

    def by_slide(value):
        return [jnp.sum(value[m * slide_rows : (m + 1) * slide_rows], axis=0, keepdims=True) for m in range(slides)]

    mass_parts = by_slide(valid * mass)
    cell_parts = by_slide(kcell)
    lane = lax.broadcasted_iota(jnp.int32, (1, LANES), 1)
    scalars = jnp.zeros((1, LANES), F32)
    for at, value in enumerate(mass_parts + cell_parts):
        scalars = jnp.where(lane == at, value, scalars)
    for m in range(slides):
        pltpu.make_async_copy(spatial_ref.at[m], tg.at[half(m)], loc.at[slides + m]).wait()

    head = backward_widths[0]
    t0[q] = tg[:, 0:head]
    for p in mates:
        send(t0.at[q], t0.at[q], t0_s, t0_r.at[q], mate(p))
    sacc[...] = jnp.zeros_like(sacc)
    s1[q, 3 * slides :, :] = jnp.zeros((8 - 3 * slides, genes), F32)
    s1[q, 3 * slides : 3 * slides + 1, 0:LANES] = scalars

    def share_logits():
        for p in (mates[1], mates[2], mates[0]):
            here = ab.at[p, half(core)]
            arrived(here, a_r.at[p])
            send(here, here, a2_s, a2_r.at[p], sibling)

    def lay_probs(p, at, value):
        af[p, at, :] = value
        there = pl.ds(pl.multiple_of(p * rows + at.start, BLOCK), BLOCK)
        probs_3[there, :] = threefold(value)

    def take_probs():
        in_blocks(0, rows, lambda at: lay_probs(q, at, pq[q, at, :]))
        for p in (mates[1], mates[2], mates[0]):
            arrived(rs.at[p], r_r.at[p])
            arrived(ab.at[p, half(1 - core)], a2_r.at[p])
            rowv[1] = jnp.concatenate([rs[p].T, jnp.zeros((rows, LANES - 8), F32)], axis=1)

            def take(at):
                probs = jnp.exp(ab[p, at, :] - rowv[1, at, 0:1]) * rowv[1, at, 1:2]
                lay_probs(p, at, probs)

            in_blocks(0, rows, take)

    def transpose(part):
        @pl.loop(0, PLANE // 2)
        def _(step):
            p = part * (PLANE // 2) + step
            high, low_part = halves(af[p].T)
            for third, value in enumerate((high, high, low_part)):
                turned_3[:, pl.ds(pl.multiple_of(third * PLANE * rows + p * rows, rows), rows)] = value

    def in_blocks(start, count, body):
        @pl.loop(0, count // BLOCK)
        def _(step):
            body(pl.ds(pl.multiple_of(start + step * BLOCK, BLOCK), BLOCK))

    quarter = lines * cb

    def lay_factor(at, length, width, value):
        high, low_part = halves(value)
        for third, part in enumerate((high, low_part, high)):
            here = pl.ds(pl.multiple_of(third * length + at.start, BLOCK), BLOCK)
            factor[here, 0:width] = part

    def keep_expr(k, at, value):
        start = sum(forward_widths[:k])
        for turn in range(turns):
            origin, width = sum(backward_widths[:turn]), backward_widths[turn]
            lo, hi = max(start, origin), min(start + forward_widths[k], origin + width)
            if lo < hi:
                high, low_part = halves(value[:, lo - start : hi - start])
                for third, part in enumerate((high, low_part, high)):
                    expr_3[at, pl.ds(3 * origin + third * width + lo - origin, hi - lo)] = part

    def three_turn_cols(k):
        return pl.ds(3 * sum(backward_widths[:k]), 3 * backward_widths[k])

    def forward_product(k):
        width = forward_widths[k]

        def lay(at):
            value = bb[k][at, :]
            lay_factor(at, quarter, width, value)
            keep_expr(k, at, value)

        in_blocks(0, quarter, lay)
        if k < chunks - 1:

            @pl.loop(0, PLANE * rows // TALL)
            def _(step):
                tall = pl.ds(pl.multiple_of(step * TALL, TALL), TALL)
                cs[k][tall, :] = product(probs_3[tall, :], factor[0 : 3 * quarter, 0:width], ((1,), (0,)))

            for p in mates:
                pass_pred(k, p)
        else:
            for side, served in ((1 - row, (mates[0], mates[2])), (row, (mates[1],))):
                pair = pl.ds(pl.multiple_of(2 * side * rows, 2 * rows), 2 * rows)
                cs[k][pair, :] = product(probs_3[pair, :], factor[0 : 3 * quarter, 0:width], ((1,), (0,)))
                for p in served:
                    pass_pred(k, p)

    def pass_pred(k, p):
        send(cs[k].at[share(p)], cr[k].at[q], c_s.at[k], c_r.at[k, q], mate(p))

    def finish_pred(k):
        total = cs[k][share(q), :]
        for p in mates:
            arrived(cr[k].at[p], c_r.at[k, p])
            total = total + cr[k][p]
        pr[:, cols(k)] = total
        if k == 0:
            p0[q] = total[:, 0:head]
            for p in mates:
                send(p0.at[q], p0.at[q], p0_s, p0_r.at[q], mate(p))
        truth = tg[:, cols(k)]
        for at, value in enumerate((total * truth, total * total, truth * truth)):
            sacc[at] += lane_groups(value)
        kept = valid * total
        stats = by_slide(kept * truth) + by_slide(kept * total) + by_slide(valid * truth * truth)
        s1[q, 0 : 3 * slides, cols(k)] = jnp.concatenate(stats, axis=0)

    early = sum(forward_widths[:EARLY])
    parts = (pl.ds(0, early), pl.ds(early, genes - early))

    def sum_plane(at):
        for p in mates:
            send(s1.at[q, :, parts[at]], s1.at[q, :, parts[at]], s1_s, s1_r.at[at, q], mate(p))

    def sum_line(at):
        for p in mates:
            arrived(s1.at[p, :, parts[at]], s1_r.at[at, p])
        s2[z, :, parts[at]] = (s1[0, :, parts[at]] + s1[1, :, parts[at]]) + (s1[2, :, parts[at]] + s1[3, :, parts[at]])
        for o in others:
            send(s2.at[z, :, parts[at]], s2.at[z, :, parts[at]], s2_s, s2_r.at[at, z], (o * PLANE + q, core))

    kept = {}

    def finish_genes(at):
        for o in others:
            arrived(s2.at[o, :, parts[at]], s2_r.at[at, o])
        total = s2[0, :, parts[at]]
        for line in range(1, lines):
            total = total + s2[line, :, parts[at]]
        gene_dot, gene_pred, gene_true = total[0:2], total[2:4], total[4:6]
        gene_inv = lax.rsqrt(gene_pred * gene_true + tiny)
        cos_gene = gene_dot * gene_inv
        gv[0:2, parts[at]] = gene_inv
        gv[2:4, parts[at]] = cos_gene * gene_true / (gene_pred * gene_true + tiny)
        kept["genes", at] = jnp.sum(jnp.sum(cos_gene, axis=1, keepdims=True), axis=0, keepdims=True)
        if at == 0:
            kept["mass"] = jnp.where(first, total[6:7, 0:1], total[6:7, 1:2])
            kept["cells"] = jnp.where(first, total[6:7, 2:3], total[6:7, 3:4])

    def sum_cores():
        sums = [jnp.sum(sacc[at], axis=1, keepdims=True) for at in range(3)]
        ss[q, core] = jnp.where(wide == 0, sums[0], jnp.where(wide == 1, sums[1], sums[2])).T[0:8]
        here = ss.at[q, core]
        send(here, here, ss_s.at[0], ss_r.at[q, core], sibling)
        for p in mates:
            send(here, here, ss_s.at[1], ss_r.at[q, core], mate(p))
            send(here, here, ss_s.at[1], ss_r.at[q, core], across(p))
        sacc[0] = jnp.zeros_like(sacc[0])

    def finish_spots():
        arrived(ss.at[q, 1 - core], ss_r.at[q, 1 - core])
        for p in mates:
            for side in range(2):
                arrived(ss.at[p, side], ss_r.at[p, side])
        lane_id = lax.broadcasted_iota(jnp.int32, (1, rows), 1)
        first_lane = lane_id < slide_rows
        lane_spot = jnp.where(first_lane, lane_id, lane_id - slide_rows)
        lane_count = jnp.where(first_lane, count_ref[0], count_ref[1])
        for p in range(PLANE):
            lane_valid = ((z * PLANE + p) * slide_rows + lane_spot < lane_count).astype(F32)
            spot = ss[p, 0] + ss[p, 1]
            spot_dot, spot_pred, spot_true = spot[0:1], spot[1:2], spot[2:3]
            spot_inv = lax.rsqrt(spot_pred * spot_true + tiny)
            cos_spot = spot_dot * spot_inv
            spot_back = cos_spot * spot_true / (spot_pred * spot_true + tiny)
            vectors = [lane_valid * spot_inv, lane_valid * spot_back, lane_valid, lane_valid * cos_spot]
            vr[p] = jnp.concatenate(vectors + [jnp.zeros((4, rows), F32)], axis=0)
        kept["cos"] = jnp.sum(vr[q, 3:4, :], axis=1, keepdims=True)

    def gradient(truth, guess, by_row, k):
        pieces = []
        for m in range(slides):
            lo, hi = m * slide_rows, (m + 1) * slide_rows
            inverse, back = gv[m : m + 1, turn_cols(k)], gv[2 + m : 3 + m, turn_cols(k)]
            spot_inv, spot_back, spot_valid = by_row[lo:hi, 0:1], by_row[lo:hi, 1:2], by_row[lo:hi, 2:3]
            pieces.append(
                guess[lo:hi] * (spot_valid * back + spot_back) - truth[lo:hi] * (spot_valid * inverse + spot_inv)
            )
        return jnp.concatenate(pieces, axis=0)

    def head_gradient():
        for p in mates:
            arrived(t0.at[p], t0_r.at[p])
            arrived(p0.at[p], p0_r.at[p])
        for p in range(PLANE):
            ds[0][share(p), :] = gradient(t0[p], p0[p], vr[p].T, 0)
        sacc[0] += lane_groups(ds[0][share(q), :] * p0[q])

    def send_grad(k):
        if k == 0:
            kept["by_row"] = vr[q].T
            return
        grad = gradient(tg[:, turn_cols(k)], pr[:, turn_cols(k)], kept["by_row"], k)
        here = ds[k].at[share(q)]
        here[...] = grad
        for p in mates:
            send(here, here, d_s.at[k], d_r.at[k, q], mate(p))
        sacc[0] += lane_groups(grad * pr[:, turn_cols(k)])

    def send_terms():
        mass_total, cell_total = kept["mass"], kept["cells"]
        portion = kcell / cell_total
        kl_rows = portion * (jnp.log(counted) - jnp.log(cell_total) - jnp.log(mass) + jnp.log(mass_total))
        dmass = scale_count * valid * (1.0 / mass_total - portion / mass)
        terms = jnp.sum(scale_count * kl_rows, axis=0, keepdims=True) - kept["cos"]
        l1[q] = jnp.broadcast_to(terms, (8, LANES))
        for p in mates:
            send(l1.at[q], l1.at[q], l1_s, l1_r.at[q], mate(p))
        inner = jnp.sum(sacc[0], axis=1, keepdims=True)
        inn[core] = jnp.where(wide == 0, inner, kept["genes", 0] + kept["genes", 1])
        send(inn.at[core], inn.at[core], in_s, in_r, sibling)
        rowv[1] = jnp.broadcast_to(dmass, (rows, LANES))

    middle = lines // 2

    def backward_product(k):
        if k == 0:
            head_gradient()
        else:
            for p in mates:
                arrived(ds[k].at[share(p)], d_r.at[k, p])
        width, spots = backward_widths[k], PLANE * rows

        def lay(at):
            value = ds[k][at, :]
            lay_factor(at, spots, width, value)
            grad_3[at, three_turn_cols(k)] = threefold(value)

        in_blocks(0, spots, lay)
        if not halved(k):

            @pl.loop(0, quarter // TALL)
            def _(step):
                tall = pl.ds(pl.multiple_of(step * TALL, TALL), TALL)
                es[k][tall, :] = product(turned_3[tall, :], factor[0 : 3 * spots, 0:width], ((1,), (0,)))

        for turn in range(2):
            if halved(k):
                side = (1 - z // middle) if turn == 0 else z // middle
                pair = pl.ds(pl.multiple_of(side * middle * cb, middle * cb), middle * cb)
                es[k][pair, :] = product(turned_3[pair, :], factor[0 : 3 * spots, 0:width], ((1,), (0,)))

            @pl.when(z == 0)
            def _():
                if halved(k):
                    pass_up(k, middle if turn == 0 else 1, middle if turn == 0 else middle - 1, turn)
                elif whole(k):
                    if turn == 0:
                        pass_up(k, 1, last, 0)
                elif turn == 0:
                    for line in range(last, 0, -1):
                        pass_up(k, line, 1, line)

            @pl.when(z == last)
            def _():
                if halved(k):
                    pass_down(k, 0 if turn == 0 else middle, middle if turn == 0 else middle - 1, turn)
                elif whole(k):
                    if turn == 0:
                        pass_down(k, 0, last, 0)
                elif turn == 0:
                    for line in range(last):
                        pass_down(k, line, 1, line)

    def halved(k):
        return k == 0

    def whole(k):
        return 0 < k < turns - SPLIT

    def pass_up(k, line, count, slot):
        here = pl.ds(line * cb, count * cb)
        send(es[k].at[here], ru[k].at[here], ru_s.at[k], ru_r.at[k, slot], up)

    def pass_down(k, line, count, slot):
        here = pl.ds(line * cb, count * cb)
        send(es[k].at[here], rd[k].at[here], rd_s.at[k], rd_r.at[k, slot], down)

    def take_up(k, line, count, slot):
        arrived(ru[k].at[pl.ds(line * cb, count * cb)], ru_r.at[k, slot])

    def take_down(k, line, count, slot):
        arrived(rd[k].at[pl.ds(line * cb, count * cb)], rd_r.at[k, slot])

    def add_up(k, line, count):
        def add(at):
            es[k][at, :] += ru[k][at, :]

        in_blocks(line * cb, count * cb, add)

    def add_down(k, line, count):
        def add(at):
            es[k][at, :] += rd[k][at, :]

        in_blocks(line * cb, count * cb, add)

    def rising(k, at):
        if halved(k) or whole(k):
            start = middle if halved(k) else at
            take_up(k, start, lines - start, 0)
            above = max(at + 1, start)
            add_up(k, above, lines - above)
            pass_up(k, above, lines - above, 0)
        else:
            for line in range(last, at, -1):
                take_up(k, line, 1, line)
                add_up(k, line, 1)
                pass_up(k, line, 1, line)

    def falling(k, at):
        if halved(k) or whole(k):
            end = middle if halved(k) else at + 1
            take_down(k, 0, end, 0)
            below = min(at, end)
            add_down(k, 0, below)
            pass_down(k, 0, below, 0)
        else:
            for line in range(at):
                take_down(k, line, 1, line)
                add_down(k, line, 1)
                pass_down(k, line, 1, line)

    def add_near(k):
        for at in range(1, last):

            @pl.when(z == at)
            def _():
                (rising if low(at) else falling)(k, at)

    def add_far(k):
        for at in range(1, last):

            @pl.when(z == at)
            def _():
                (falling if low(at) else rising)(k, at)

    def finish_expr(k):
        for at in range(lines):

            @pl.when(z == at)
            def _():
                if at > 0:
                    if halved(k) and at < middle:
                        take_up(k, at, 1, 1)
                    elif at == last and (halved(k) or whole(k)):
                        take_up(k, at, 1, 0)
                    elif not halved(k) and not whole(k):
                        take_up(k, at, 1, at)
                if at < last:
                    if halved(k) and at >= middle:
                        take_down(k, at, 1, 1)
                    elif at == 0 and (halved(k) or whole(k)):
                        take_down(k, at, 1, 0)
                    elif not halved(k) and not whole(k):
                        take_down(k, at, 1, at)

        from_low, from_high = z > 0, z < last

        @pl.loop(0, cb // BLOCK)
        def _(step):
            here = pl.ds(pl.multiple_of(step * BLOCK, BLOCK), BLOCK)
            own = pl.ds(pl.multiple_of(z * cb + step * BLOCK, BLOCK), BLOCK)
            total = es[k][own, :]
            total = total + jnp.where(from_low, ru[k][own, :], 0.0)
            ge[here, turn_cols(k)] = total + jnp.where(from_high, rd[k][own, :], 0.0)

    def probs_gradient(k):
        at = three_turn_cols(k)

        @pl.loop(0, PLANE * rows // TALL)
        def _(step):
            tall = pl.ds(pl.multiple_of(step * TALL, TALL), TALL)
            part = product(grad_3[tall, at], expr_3[:, at], ((1,), (1,)))
            if k == 0:
                fs[tall, :] = part
            else:
                fs[tall, :] += part

    def slide_of(p, m):
        return pl.ds(pl.multiple_of(p * rows + m * slide_rows, slide_rows), slide_rows)

    def sum_probs_cores():
        for p in mates + (q,):
            fx[p] = fs[slide_of(p, 1 - core), :]
            send(fx.at[p], fy.at[p], fx_s, fx_r.at[p], sibling)

    def return_probs():
        for p in mates:
            arrived(fy.at[p], fx_r.at[p])
            fz[p] = fs[slide_of(p, core), :] + fy[p]
            send(fz.at[p], fr.at[q], f_s, f_r.at[q], mate(p))
        arrived(fy.at[q], fx_r.at[q])
        fr[q] = fs[slide_of(q, core), :] + fy[q]

    def pass_terms():
        for p in mates:
            arrived(l1.at[p], l1_r.at[p])
        l2[z] = (l1[0] + l1[1]) + (l1[2] + l1[3])
        for o in others:
            send(l2.at[z], l2.at[z], l2_s, l2_r.at[z], (o * PLANE + q, core))

    def part_of(slide, m):
        start = slide * slide_rows + m * (slide_rows // 2)
        return pl.ds(pl.multiple_of(start, slide_rows // 2), slide_rows // 2)

    def finish_logits():
        arrived(inn.at[1 - core], in_r)
        rowv[2] = (inn[0] + inn[1]) + rowv[1] * rowv[0]
        for p in mates:
            arrived(fr.at[p], f_r.at[p])
        for m in range(2):

            @pl.loop(0, slide_rows // STEP_ROWS // 2)
            def _(step):
                row_at = (m * (slide_rows // STEP_ROWS // 2) + step) * STEP_ROWS
                at = pl.ds(pl.multiple_of(row_at, STEP_ROWS), STEP_ROWS)
                whole_at = pl.ds(pl.multiple_of(core * slide_rows + row_at, STEP_ROWS), STEP_ROWS)
                by_mass, total_inner = rowv[1, whole_at, 0:1], rowv[2, whole_at, 0:1]
                for p in range(PLANE):
                    for line in range(lines):
                        here, there = pl.ds(line * cb, cb), (line * PLANE + p) * cb
                        grad = fr[p, at, here] + by_mass * weights[:, there : there + cb]
                        glog[whole_at, pl.ds(there, cb)] = pq[p, whole_at, here] * (grad - total_inner)

            here = part_of(core, m)
            send(glog.at[here], glog.at[here], go_s, go_r.at[m], sibling)

    def forward_left():
        for k in range(chunks):

            @pl.when(z < last)
            def _():
                sent(bb[k].at[block(z)], ou_s.at[k])

            @pl.when(z > 0)
            def _():
                sent(bb[k].at[block(z)], od_s.at[k])

            for at in range(1, last):

                @pl.when(z == at)
                def _():
                    sent(bb[k].at[pl.ds(0, at * cb)], fu_s.at[k])
                    sent(bb[k].at[pl.ds((at + 1) * cb, (last - at) * cb)], fd_s.at[k])

        three = pl.ds(0, len(mates))
        sent(ab.at[three, half(0)], a_s)
        sent(ab.at[three, half(0)], a2_s)
        sent(rs.at[three], r_s)
        sent(t0.at[three], t0_s)
        sent(p0.at[three], p0_s)
        for k in range(chunks):
            sent(cr[k].at[three], c_s.at[k])
        sent(s1.at[three], s1_s)
        sent(s2.at[pl.ds(0, last)], s2_s)
        sent(ss.at[0, 0], ss_s.at[0])
        sent(ss.at[three], ss_s.at[1])

    steps = {
        "far": forward_far,
        "near": forward_near,
        "share": share_logits,
        "take": take_probs,
        "whole": gathered,
        "product": forward_product,
        "sum": finish_pred,
        "turn": transpose,
        "plane": sum_plane,
        "line": sum_line,
        "genes": finish_genes,
        "cores": sum_cores,
        "spots": finish_spots,
        "grad": send_grad,
        "terms": send_terms,
        "backward": backward_product,
        "probs": probs_gradient,
        "exchange": sum_probs_cores,
        "return": return_probs,
        "loss": pass_terms,
        "logits": finish_logits,
        "add_near": add_near,
        "add_far": add_far,
        "expr": finish_expr,
        "left": forward_left,
    }
    for name, *where in STEPS:
        steps[name](*where)

    for o in others:
        arrived(l2.at[o], l2_r.at[o])
    loss = l2[0]
    for line in range(1, lines):
        loss = loss + l2[line]
    loss_ref[...] = loss[0:1, 0:1] - (inn[0, 0:1, 1:2] + inn[1, 0:1, 1:2])
    for m in range(2):
        arrived(glog.at[part_of(1 - core, m)], go_r.at[m])

    for k in range(turns):
        for at in range(lines):

            @pl.when(z == at)
            def _():
                if at < last:
                    sent(es[k].at[pl.ds((at + 1) * cb, (last - at) * cb)], ru_s.at[k])
                if at > 0:
                    sent(es[k].at[pl.ds(0, at * cb)], rd_s.at[k])

    three = pl.ds(0, len(mates))
    for k in range(1, turns):
        sent(ds[k].at[pl.ds(0, len(mates) * rows)], d_s.at[k])
    sent(inn.at[0], in_s)
    sent(l1.at[three], l1_s)
    sent(l2.at[pl.ds(0, last)], l2_s)
    sent(fr.at[three], f_s)
    sent(fx, fx_s)
    sent(glog.at[half(0)], go_s)


def lane_groups(value):
    parts = [value[:, at : at + LANES] for at in range(0, value.shape[1], LANES)]
    return functools.reduce(lambda a, b: a + b, parts)


def grouped(refs, sizes):
    at = 0
    for size in sizes:
        yield refs[at : at + size]
        at += size


def deliver(pred_in, loss_in, glog_in, gexp_in, pred_ref, loss_ref, glog_ref, gexp_ref, sems):
    slides, slide_rows = pred_ref.shape[0], pred_ref.shape[1]
    pairs = [(gexp_in, gexp_ref), (loss_in, loss_ref)]
    for m in range(slides):
        part = pl.ds(m * slide_rows, slide_rows)
        pairs += [(glog_in.at[part], glog_ref.at[m]), (pred_in.at[part], pred_ref.at[m])]
    copies = [pltpu.make_async_copy(src, dst, sems.at[at]) for at, (src, dst) in enumerate(pairs)]
    for copy in copies:
        copy.start()
    for copy in copies:
        copy.wait()


def plane_call(logits, expr, spatial, slide_spots, spot_cells, cell_prior, lines):
    slides, slide_rows, cells = logits.shape
    rows = slides * slide_rows
    cb, genes = expr.shape
    quarter = lines * cb
    spots = PLANE * rows
    chunks, turns = len(FORWARD), len(BACKWARD)
    dma = pltpu.SemaphoreType.DMA
    vmem = pltpu.VMEM
    anywhere = pl.BlockSpec(memory_space=pl.ANY)
    in_vmem = pl.BlockSpec(memory_space=pltpu.VMEM)
    scratch = [
        pltpu.SMEM((slides,), jnp.int32),
        vmem((slides, slide_rows), jnp.int32),
        vmem((1, cells), jnp.int32),
        vmem((rows, cells), F32),
        vmem((PLANE, slide_rows, quarter), F32),
        vmem((rows, genes), F32),
        vmem((cb, genes), F32),
        vmem((PLANE, rows, quarter), F32),
        vmem((PLANE, rows, quarter), F32),
        vmem((PLANE, rows, quarter), F32),
        vmem((spots, 3 * quarter), BF16),
        vmem((quarter, 3 * spots), BF16),
        vmem((quarter, 3 * genes), BF16),
        vmem((3, rows, LANES), F32),
        vmem((PLANE, 8, genes), F32),
        vmem((lines, 8, genes), F32),
        vmem((8, genes), F32),
        vmem((PLANE, 2, 8, rows), F32),
        vmem((3, rows, LANES), F32),
        vmem((PLANE, 8, rows), F32),
        vmem((spots, 3 * genes), BF16),
        vmem((3 * max(quarter, spots), max(FORWARD + BACKWARD)), BF16),
        vmem((PLANE, rows, BACKWARD[0]), F32),
        vmem((PLANE, rows, BACKWARD[0]), F32),
        vmem((PLANE, 8, rows), F32),
        vmem((spots, quarter), F32),
        vmem((PLANE, slide_rows, quarter), F32),
        vmem((PLANE, slide_rows, quarter), F32),
        vmem((PLANE, slide_rows, quarter), F32),
        vmem((PLANE, slide_rows, quarter), F32),
        vmem((2, rows, LANES), F32),
        vmem((PLANE, 8, LANES), F32),
        vmem((lines, 8, LANES), F32),
        dma((2 * slides + 4,)),
        dma((chunks,)),
        dma((chunks,)),
        dma((chunks,)),
        dma((chunks,)),
        dma((chunks,)),
        dma((chunks,)),
        dma((chunks,)),
        dma((chunks,)),
        dma,
        dma((PLANE,)),
        dma,
        dma((PLANE,)),
        dma,
        dma((PLANE,)),
        dma((chunks,)),
        dma((chunks, PLANE)),
        dma,
        dma((2, PLANE)),
        dma,
        dma((2, lines)),
        dma((2,)),
        dma((PLANE, 2)),
        dma((turns,)),
        dma((turns, PLANE)),
        dma((turns,)),
        dma((turns, lines)),
        dma((turns,)),
        dma((turns, lines)),
        dma,
        dma((PLANE,)),
        dma,
        dma((PLANE,)),
        dma,
        dma((2,)),
        dma,
        dma,
        dma,
        dma((PLANE,)),
        dma,
        dma((lines,)),
        dma,
        dma((PLANE,)),
        dma,
        dma((PLANE,)),
    ]
    for shape, widths in (
        ((quarter,), FORWARD),
        ((spots,), FORWARD),
        ((PLANE, rows), FORWARD),
        ((spots,), BACKWARD),
        ((quarter,), BACKWARD),
        ((quarter,), BACKWARD),
        ((quarter,), BACKWARD),
    ):
        scratch += [vmem(shape + (width,), F32) for width in widths]
    in_hbm = functools.partial(pltpu.with_memory_space_constraint, memory_space=pltpu.HBM)
    in_place = functools.partial(pltpu.with_memory_space_constraint, memory_space=pltpu.VMEM)
    results = pl.pallas_call(
        functools.partial(plane_kernel, lines, FORWARD, BACKWARD),
        out_shape=(
            vmem((rows, genes), F32),
            vmem((1, 1), F32),
            vmem((rows, cells), F32),
            vmem((cb, genes), F32),
        ),
        in_specs=[anywhere] * 6,
        out_specs=(in_vmem,) * 4,
        scratch_shapes=scratch,
        compiler_params=pltpu.CompilerParams(
            collective_id=0, has_side_effects=True, vmem_limit_bytes=48 * 1024 * 1024
        ),
    )(*map(in_hbm, (logits, expr, spatial, slide_spots, spot_cells, cell_prior.reshape(1, cells))))
    pred, loss, grad_logits, grad_expr = pl.pallas_call(
        deliver,
        out_shape=(
            jax.ShapeDtypeStruct((slides, slide_rows, genes), F32),
            jax.ShapeDtypeStruct((1, 1), F32),
            jax.ShapeDtypeStruct((slides, slide_rows, cells), F32),
            jax.ShapeDtypeStruct((cb, genes), F32),
        ),
        in_specs=[anywhere] * 4,
        out_specs=(anywhere,) * 4,
        scratch_shapes=[dma((2 * slides + 2,))],
        compiler_params=pltpu.CompilerParams(vmem_limit_bytes=4 * 1024 * 1024),
    )(*map(in_place, results))
    return pred, loss.reshape(()), grad_logits, grad_expr


def general_plan(logits, expr, spatial, slide_spots, spot_cells, cell_prior):
    place = lax.axis_index("spot")
    side = lax.axis_index("gene")
    rows_all = logits.shape[1]
    cell_rows = expr.shape[0]
    weights = cell_prior.astype(jnp.float32) / fixed_point
    gene_share = (place == 0).astype(jnp.float32)
    row_share = (side == 0).astype(jnp.float32)
    own_weights = lax.dynamic_slice_in_dim(weights, place * cell_rows, cell_rows, 0)
    expr_acc = jnp.zeros((cell_rows, expr.shape[1]), jnp.float32)
    loss_local = jnp.zeros((), jnp.float32)
    pred_list = []
    grad_list = []
    for slide in range(logits.shape[0]):
        logit_rows = logits[slide]
        counted = spot_cells[slide].astype(jnp.float32)
        target = spatial[slide]
        positions = place * rows_all + jnp.arange(rows_all, dtype=jnp.int32)
        valid = (positions < slide_spots[slide]).astype(jnp.float32)
        peak = jnp.max(logit_rows, axis=1, keepdims=True)
        raised = jnp.exp(logit_rows - peak)
        probs = raised / jnp.sum(raised, axis=1, keepdims=True)
        mass = jnp.dot(probs, weights, precision=lax.Precision.HIGHEST)
        blocks = lax.all_to_all(probs, "spot", split_axis=1, concat_axis=0, tiled=True)
        pred = lax.psum_scatter(
            jnp.dot(blocks, expr, precision=lax.Precision.HIGHEST),
            "spot",
            scatter_dimension=0,
            tiled=True,
        )
        gene_dot = jnp.sum(valid[:, None] * pred * target, axis=0)
        gene_pred = jnp.sum(valid[:, None] * pred * pred, axis=0)
        gene_true = jnp.sum(valid[:, None] * target * target, axis=0)
        mass_part = jnp.sum(valid * mass)
        kcell = valid * counted
        cell_part = jnp.sum(kcell)
        spot_dot = jnp.sum(pred * target, axis=1)
        spot_pred = jnp.sum(pred * pred, axis=1)
        spot_true = jnp.sum(target * target, axis=1)
        gene_dot, gene_pred, gene_true, mass_total, cell_total = lax.psum(
            (gene_dot, gene_pred, gene_true, mass_part, cell_part), "spot"
        )
        spot_dot, spot_pred, spot_true = lax.psum((spot_dot, spot_pred, spot_true), "gene")
        gene_inv = lax.rsqrt(gene_pred * gene_true + tiny)
        cos_gene = gene_dot * gene_inv
        spot_inv = lax.rsqrt(spot_pred * spot_true + tiny)
        cos_spot = spot_dot * spot_inv
        share = kcell / cell_total
        scale_count = slide_spots[slide].astype(jnp.float32)
        kl_part = jnp.sum(
            share * (jnp.log(counted) - jnp.log(cell_total) - jnp.log(mass) + jnp.log(mass_total))
        )
        loss_local = loss_local - gene_share * jnp.sum(cos_gene)
        loss_local = loss_local + row_share * (scale_count * kl_part - jnp.sum(valid * cos_spot))
        gene_back = cos_gene * gene_true / (gene_pred * gene_true + tiny)
        spot_back = cos_spot * spot_true / (spot_pred * spot_true + tiny)
        dpred = -valid[:, None] * (
            target * (gene_inv[None, :] + spot_inv[:, None])
            - pred * gene_back[None, :]
            - pred * spot_back[:, None]
        )
        dmass = scale_count * valid * (1.0 / mass_total - share / mass)
        pred_list.append(pred)
        grads_full, mass_full = (
            lax.all_gather(dpred, "spot", axis=0, tiled=True),
            lax.all_gather(dmass, "spot", axis=0, tiled=True),
        )
        dprob_cells = jnp.dot(grads_full, expr.T, precision=lax.Precision.HIGHEST)
        dprob_cells = lax.psum(dprob_cells, "gene")
        expr_acc = expr_acc + lax.dot_general(
            blocks, grads_full, (((0,), (0,)), ((), ())), precision=lax.Precision.HIGHEST
        )
        dprob_cells = dprob_cells + mass_full[:, None] * own_weights[None, :]
        dprob_rows = lax.all_to_all(dprob_cells, "spot", split_axis=0, concat_axis=1, tiled=True)
        inner = jnp.sum(probs * dprob_rows, axis=1, keepdims=True)
        dlogit = probs * (dprob_rows - inner)
        grad_list.append(dlogit)
    loss = lax.psum(loss_local, ("spot", "gene"))
    return (jnp.stack(pred_list), loss, jnp.stack(grad_list), expr_acc)


def solution(mesh):
    places = mesh.shape["spot"]

    def on_device(logits, expr, spatial, slide_spots, spot_cells, cell_prior):
        if places == PLANE * PLANE and mesh.shape["gene"] == 2 and expr.shape[1] == sum(FORWARD):
            return plane_call(
                logits, expr, spatial, slide_spots, spot_cells, cell_prior, places // PLANE
            )
        return general_plan(logits, expr, spatial, slide_spots, spot_cells, cell_prior)

    in_specs = (
        P(None, "spot", None),
        P("spot", "gene"),
        P(None, "spot", "gene"),
        P(),
        P(None, "spot"),
        P(),
    )
    out_specs = (P(None, "spot", "gene"), P(), P(None, "spot", None), P("spot", "gene"))
    return jax.shard_map(
        on_device, mesh=mesh, in_specs=in_specs, out_specs=out_specs, check_vma=False
    )
```

```python
import functools

import jax
import jax.numpy as jnp
from jax import lax
from jax.experimental import pallas as pl
from jax.experimental.pallas import tpu as pltpu
from jax.sharding import PartitionSpec as P

tiny = 1e-06
fixed_point = 16384.0
F32 = jnp.float32
BF16 = jnp.bfloat16
MESH = pl.DeviceIdType.MESH

PLANE = 4
LANES = 128
STEP_ROWS = 16
BLOCK = 32
TALL = 256
FORWARD = (128, 256, 256, 256, 128)
BACKWARD = (128, 128, 256, 256, 256)
SPLIT = 2
LEAD = 2
NEAR_LEAD = 3
EARLY = 3
STEPS = (
    ("far", 0),
    ("far", 1),
    ("near", 0),
    ("share",),
    ("far", 2),
    ("far", 3),
    ("take",),
    ("whole", 0),
    ("near", 1),
    ("product", 0),
    ("sum", 0),
    ("whole", 1),
    ("near", 2),
    ("product", 1),
    ("whole", 2),
    ("product", 2),
    ("whole", 3),
    ("near", 3),
    ("product", 3),
    ("whole", 4),
    ("far", 4),
    ("near", 4),
    ("product", 4),
    ("turn", 0),
    ("sum", 1),
    ("sum", 2),
    ("plane", 0),
    ("turn", 1),
    ("sum", 3),
    ("line", 0),
    ("sum", 4),
    ("plane", 1),
    ("cores",),
    ("genes", 0),
    ("spots",),
    ("grad", 0),
    ("grad", 1),
    ("grad", 2),
    ("line", 1),
    ("backward", 0),
    ("backward", 1),
    ("add_near", 0),
    ("genes", 1),
    ("grad", 3),
    ("backward", 2),
    ("probs", 0),
    ("add_far", 0),
    ("probs", 1),
    ("expr", 0),
    ("grad", 4),
    ("add_near", 1),
    ("probs", 2),
    ("terms",),
    ("backward", 3),
    ("probs", 3),
    ("add_near", 2),
    ("backward", 4),
    ("add_far", 1),
    ("probs", 4),
    ("exchange",),
    ("add_near", 3),
    ("add_far", 2),
    ("left",),
    ("return",),
    ("loss",),
    ("add_far", 3),
    ("expr", 1),
    ("add_near", 4),
    ("logits",),
    ("add_far", 4),
    ("expr", 2),
    ("expr", 3),
    ("expr", 4),
)


def halves(value):
    high = value.astype(BF16)
    return high, (value - high.astype(F32)).astype(BF16)


def threefold(value):
    high, low = halves(value)
    return jnp.concatenate([high, high, low], axis=1)


def product(a, b, contract):
    return lax.dot_general(a, b, (contract, ((), ())), preferred_element_type=F32)


def plane_kernel(lines, forward_widths, backward_widths, *refs):
    chunks, turns = len(forward_widths), len(backward_widths)
    (
        (logits_ref, expr_ref, spatial_ref, count_in, cells_in, prior_in),
        (pr, loss_ref, glog, ge),
        (count_ref, cells_ref, prior_ref, lg, lq, tg, ex, pq, ab, af, probs_3, turned_3, expr_3, sacc, s1, s2, gv, ss, rowv, rs),
        (grad_3, factor, t0, p0, vr, fs, fx, fy, fz, fr, inn, l1, l2),
        (loc, ou_s, ou_r, od_s, od_r, fu_s, fu_r, fd_s, fd_r, a_s, a_r, a2_s, a2_r, r_s, r_r),
        (c_s, c_r, s1_s, s1_r, s2_s, s2_r, ss_s, ss_r, d_s, d_r, ru_s, ru_r, rd_s, rd_r),
        (f_s, f_r, fx_s, fx_r, go_s, go_r, in_s, in_r, l1_s, l1_r, l2_s, l2_r, t0_s, t0_r, p0_s, p0_r, vr_s, vr_r),
        bb,
        cs,
        cr,
        ds,
        es,
        ru,
        rd,
    ) = grouped(refs, (6, 4, 20, 13, 15, 14, 18, chunks, chunks, chunks, turns, turns, turns, turns))
    place = lax.axis_index("spot")
    core = lax.axis_index("gene")
    z = place // PLANE
    q = place % PLANE
    col, row = q % 2, q // 2
    mates = ((1 - row) * 2 + 1 - col, row * 2 + 1 - col, (1 - row) * 2 + col)
    others = tuple((z + step) % lines for step in range(1, lines))
    up, down = (place + PLANE, core), (place - PLANE, core)
    sibling = (place, 1 - core)
    slides, slide_rows = logits_ref.shape[0], logits_ref.shape[1]
    rows = slides * slide_rows
    cb = expr_ref.shape[0]
    genes = expr_ref.shape[1]
    last = lines - 1

    def mate(p):
        return (z * PLANE + p, core)

    def send(src, dst, send_sem, recv_sem, device):
        copy = pltpu.make_async_remote_copy(
            src_ref=src, dst_ref=dst, send_sem=send_sem, recv_sem=recv_sem, device_id=device, device_id_type=MESH
        )
        copy.start()

    def arrived(dst, recv_sem):
        pltpu.make_async_copy(dst, dst, recv_sem).wait()

    sent = arrived

    def cols(k):
        return pl.ds(sum(forward_widths[:k]), forward_widths[k])

    def turn_cols(k):
        return pl.ds(sum(backward_widths[:k]), backward_widths[k])

    def block(index):
        return pl.ds(pl.multiple_of(index * cb, cb), cb)

    def share(index):
        return pl.ds(pl.multiple_of(index * rows, rows), rows)

    def half(index):
        return pl.ds(pl.multiple_of(index * slide_rows, slide_rows), slide_rows)

    small = ((prior_in, prior_ref), (count_in, count_ref), (cells_in, cells_ref))
    pltpu.make_async_copy(expr_ref, ex, loc.at[2 * slides]).start()
    for m in range(slides):
        pltpu.make_async_copy(logits_ref.at[m], lg.at[half(m)], loc.at[m]).start()
    for at, (src, dst) in enumerate(small):
        pltpu.make_async_copy(src, dst, loc.at[2 * slides + 1 + at]).start()
    for m in range(slides):
        pltpu.make_async_copy(spatial_ref.at[m], tg.at[half(m)], loc.at[slides + m]).start()

    barrier = pltpu.get_barrier_semaphore()
    for p in mates:
        pl.semaphore_signal(barrier, inc=1, device_id=mate(p), device_id_type=MESH)
    for o in others:
        pl.semaphore_signal(barrier, inc=1, device_id=(o * PLANE + q, core), device_id_type=MESH)
    pl.semaphore_signal(barrier, inc=1, device_id=sibling, device_id_type=MESH)
    pltpu.make_async_copy(expr_ref, ex, loc.at[2 * slides]).wait()
    for k in range(chunks):
        bb[k][block(z), :] = ex[:, cols(k)]
    for m in range(slides):
        pltpu.make_async_copy(logits_ref.at[m], lg.at[half(m)], loc.at[m]).wait()
    for p in range(PLANE):
        for line in range(lines):
            lq[p, :, pl.ds(line * cb, cb)] = lg[half(core), pl.ds((line * PLANE + p) * cb, cb)]
    pl.semaphore_wait(barrier, len(mates) + len(others) + 1)

    def own_up(k):
        here = bb[k].at[block(z)]
        send(here, here, ou_s.at[k], ou_r.at[k], up)

    def own_down(k):
        here = bb[k].at[block(z)]
        send(here, here, od_s.at[k], od_r.at[k], down)

    def low(at):
        return 2 * at < lines

    for at in range(lines):

        @pl.when(z == at)
        def _():
            for k in range(chunks):
                if at < last and (at == 0 or k < (LEAD if low(at) else NEAR_LEAD)):
                    own_up(k)
                if at > 0 and (at == last or k < (NEAR_LEAD if low(at) else LEAD)):
                    own_down(k)

    for p in mates:
        send(lq.at[p], ab.at[q, half(core)], a_s, a_r.at[q], mate(p))

    def from_below(k, at):
        arrived(bb[k].at[pl.ds((at - 1) * cb, cb)], ou_r.at[k])
        if at > 1:
            arrived(bb[k].at[pl.ds(0, (at - 1) * cb)], fu_r.at[k])

    def from_above(k, at):
        arrived(bb[k].at[pl.ds((at + 1) * cb, cb)], od_r.at[k])
        if at < last - 1:
            arrived(bb[k].at[pl.ds((at + 2) * cb, (last - 1 - at) * cb)], fd_r.at[k])

    def upward(k, at):
        from_below(k, at)
        here = bb[k].at[pl.ds(0, at * cb)]
        send(here, here, fu_s.at[k], fu_r.at[k], up)

    def downward(k, at):
        from_above(k, at)
        here = bb[k].at[pl.ds((at + 1) * cb, (last - at) * cb)]
        send(here, here, fd_s.at[k], fd_r.at[k], down)

    def forward_far(k):
        for at in range(1, last):

            @pl.when(z == at)
            def _():
                (upward if low(at) else downward)(k, at)
                if k + LEAD < chunks:
                    (own_up if low(at) else own_down)(k + LEAD)

    def forward_near(k):
        for at in range(1, last):

            @pl.when(z == at)
            def _():
                (downward if low(at) else upward)(k, at)
                if k + NEAR_LEAD < chunks:
                    (own_down if low(at) else own_up)(k + NEAR_LEAD)

    def gathered(k):
        @pl.when(z == 0)
        def _():
            from_above(k, 0)

        @pl.when(z == last)
        def _():
            from_below(k, last)

    for at, (src, dst) in enumerate(small):
        pltpu.make_async_copy(src, dst, loc.at[2 * slides + 1 + at]).wait()
    weights = prior_ref[...].astype(F32) / fixed_point

    @pl.loop(0, rows // STEP_ROWS)
    def _(step):
        at = pl.ds(pl.multiple_of(step * STEP_ROWS, STEP_ROWS), STEP_ROWS)
        value = lg[at, :]
        peak = jnp.max(value, axis=1, keepdims=True)
        raised = jnp.exp(value - peak)
        scale = 1.0 / jnp.sum(raised, axis=1, keepdims=True)
        probs = raised * scale
        mass_rows = jnp.sum(probs * weights, axis=1, keepdims=True)
        rowv[0, at, :] = jnp.broadcast_to(mass_rows, (STEP_ROWS, LANES))
        rowv[1, at, :] = jnp.broadcast_to(peak, (STEP_ROWS, LANES))
        rowv[2, at, :] = jnp.broadcast_to(scale, (STEP_ROWS, LANES))
        for p in range(PLANE):
            for line in range(lines):
                at_cells = (line * PLANE + p) * cb
                pq[p, at, pl.ds(line * cb, cb)] = probs[:, at_cells : at_cells + cb]

    wide = lax.broadcasted_iota(jnp.int32, (rows, LANES), 1)
    rs[q] = jnp.where(wide == 0, rowv[1], rowv[2]).T[0:8]
    for p in mates:
        send(rs.at[q], rs.at[q], r_s, r_r.at[q], mate(p))

    rid = lax.broadcasted_iota(jnp.int32, (rows, 1), 0)
    first = rid < slide_rows
    position = place * slide_rows + jnp.where(first, rid, rid - slide_rows)
    count = jnp.where(first, count_ref[0], count_ref[1])
    valid = (position < count).astype(F32)
    scale_count = count.astype(F32)
    square = (slide_rows, slide_rows)
    eye = lax.broadcasted_iota(jnp.int32, square, 0) == lax.broadcasted_iota(jnp.int32, square, 1)
    counted = jnp.concatenate(
        [
            jnp.sum(jnp.where(eye, cells_ref[m : m + 1, :].astype(F32), 0.0), axis=1, keepdims=True)
            for m in range(slides)
        ],
        axis=0,
    )
    mass = rowv[0, :, 0:1]
    kcell = valid * counted

    def by_slide(value):
        return [jnp.sum(value[m * slide_rows : (m + 1) * slide_rows], axis=0, keepdims=True) for m in range(slides)]

    mass_parts = by_slide(valid * mass)
    cell_parts = by_slide(kcell)
    lane = lax.broadcasted_iota(jnp.int32, (1, LANES), 1)
    scalars = jnp.zeros((1, LANES), F32)
    for at, value in enumerate(mass_parts + cell_parts):
        scalars = jnp.where(lane == at, value, scalars)
    for m in range(slides):
        pltpu.make_async_copy(spatial_ref.at[m], tg.at[half(m)], loc.at[slides + m]).wait()

    head = backward_widths[0]
    t0[q] = tg[:, 0:head]
    for p in mates:
        send(t0.at[q], t0.at[q], t0_s, t0_r.at[q], mate(p))
    sacc[...] = jnp.zeros_like(sacc)
    s1[q, 3 * slides :, :] = jnp.zeros((8 - 3 * slides, genes), F32)
    s1[q, 3 * slides : 3 * slides + 1, 0:LANES] = scalars

    def share_logits():
        for p in (mates[1], mates[2], mates[0]):
            here = ab.at[p, half(core)]
            arrived(here, a_r.at[p])
            send(here, here, a2_s, a2_r.at[p], sibling)

    def lay_probs(p, at, value):
        af[p, at, :] = value
        there = pl.ds(pl.multiple_of(p * rows + at.start, BLOCK), BLOCK)
        probs_3[there, :] = threefold(value)

    def take_probs():
        in_blocks(0, rows, lambda at: lay_probs(q, at, pq[q, at, :]))
        for p in (mates[1], mates[2], mates[0]):
            arrived(rs.at[p], r_r.at[p])
            arrived(ab.at[p, half(1 - core)], a2_r.at[p])
            rowv[1] = jnp.concatenate([rs[p].T, jnp.zeros((rows, LANES - 8), F32)], axis=1)

            def take(at):
                probs = jnp.exp(ab[p, at, :] - rowv[1, at, 0:1]) * rowv[1, at, 1:2]
                lay_probs(p, at, probs)

            in_blocks(0, rows, take)

    def transpose(part):
        @pl.loop(0, PLANE // 2)
        def _(step):
            p = part * (PLANE // 2) + step
            high, low_part = halves(af[p].T)
            for third, value in enumerate((high, high, low_part)):
                turned_3[:, pl.ds(pl.multiple_of(third * PLANE * rows + p * rows, rows), rows)] = value

    def in_blocks(start, count, body):
        @pl.loop(0, count // BLOCK)
        def _(step):
            body(pl.ds(pl.multiple_of(start + step * BLOCK, BLOCK), BLOCK))

    quarter = lines * cb

    def lay_factor(at, length, width, value):
        high, low_part = halves(value)
        for third, part in enumerate((high, low_part, high)):
            here = pl.ds(pl.multiple_of(third * length + at.start, BLOCK), BLOCK)
            factor[here, 0:width] = part

    def keep_expr(k, at, value):
        start = sum(forward_widths[:k])
        for turn in range(turns):
            origin, width = sum(backward_widths[:turn]), backward_widths[turn]
            lo, hi = max(start, origin), min(start + forward_widths[k], origin + width)
            if lo < hi:
                high, low_part = halves(value[:, lo - start : hi - start])
                for third, part in enumerate((high, low_part, high)):
                    expr_3[at, pl.ds(3 * origin + third * width + lo - origin, hi - lo)] = part

    def three_turn_cols(k):
        return pl.ds(3 * sum(backward_widths[:k]), 3 * backward_widths[k])

    def forward_product(k):
        width = forward_widths[k]

        def lay(at):
            value = bb[k][at, :]
            lay_factor(at, quarter, width, value)
            keep_expr(k, at, value)

        in_blocks(0, quarter, lay)
        if k < chunks - 1:

            @pl.loop(0, PLANE * rows // TALL)
            def _(step):
                tall = pl.ds(pl.multiple_of(step * TALL, TALL), TALL)
                cs[k][tall, :] = product(probs_3[tall, :], factor[0 : 3 * quarter, 0:width], ((1,), (0,)))

            for p in mates:
                pass_pred(k, p)
        else:
            for side, served in ((1 - row, (mates[0], mates[2])), (row, (mates[1],))):
                pair = pl.ds(pl.multiple_of(2 * side * rows, 2 * rows), 2 * rows)
                cs[k][pair, :] = product(probs_3[pair, :], factor[0 : 3 * quarter, 0:width], ((1,), (0,)))
                for p in served:
                    pass_pred(k, p)

    def pass_pred(k, p):
        send(cs[k].at[share(p)], cr[k].at[q], c_s.at[k], c_r.at[k, q], mate(p))

    def finish_pred(k):
        total = cs[k][share(q), :]
        for p in mates:
            arrived(cr[k].at[p], c_r.at[k, p])
            total = total + cr[k][p]
        pr[:, cols(k)] = total
        if k == 0:
            p0[q] = total[:, 0:head]
            for p in mates:
                send(p0.at[q], p0.at[q], p0_s, p0_r.at[q], mate(p))
        truth = tg[:, cols(k)]
        for at, value in enumerate((total * truth, total * total, truth * truth)):
            sacc[at] += lane_groups(value)
        kept = valid * total
        stats = by_slide(kept * truth) + by_slide(kept * total) + by_slide(valid * truth * truth)
        s1[q, 0 : 3 * slides, cols(k)] = jnp.concatenate(stats, axis=0)

    early = sum(forward_widths[:EARLY])
    parts = (pl.ds(0, early), pl.ds(early, genes - early))

    def sum_plane(at):
        for p in mates:
            send(s1.at[q, :, parts[at]], s1.at[q, :, parts[at]], s1_s, s1_r.at[at, q], mate(p))

    def sum_line(at):
        for p in mates:
            arrived(s1.at[p, :, parts[at]], s1_r.at[at, p])
        s2[z, :, parts[at]] = (s1[0, :, parts[at]] + s1[1, :, parts[at]]) + (s1[2, :, parts[at]] + s1[3, :, parts[at]])
        for o in others:
            send(s2.at[z, :, parts[at]], s2.at[z, :, parts[at]], s2_s, s2_r.at[at, z], (o * PLANE + q, core))

    kept = {}

    def finish_genes(at):
        for o in others:
            arrived(s2.at[o, :, parts[at]], s2_r.at[at, o])
        total = s2[0, :, parts[at]]
        for line in range(1, lines):
            total = total + s2[line, :, parts[at]]
        gene_dot, gene_pred, gene_true = total[0:2], total[2:4], total[4:6]
        gene_inv = lax.rsqrt(gene_pred * gene_true + tiny)
        cos_gene = gene_dot * gene_inv
        gv[0:2, parts[at]] = gene_inv
        gv[2:4, parts[at]] = cos_gene * gene_true / (gene_pred * gene_true + tiny)
        kept["genes", at] = jnp.sum(jnp.sum(cos_gene, axis=1, keepdims=True), axis=0, keepdims=True)
        if at == 0:
            kept["mass"] = jnp.where(first, total[6:7, 0:1], total[6:7, 1:2])
            kept["cells"] = jnp.where(first, total[6:7, 2:3], total[6:7, 3:4])

    def sum_cores():
        sums = [jnp.sum(sacc[at], axis=1, keepdims=True) for at in range(3)]
        ss[core] = jnp.where(wide == 0, sums[0], jnp.where(wide == 1, sums[1], sums[2])).T[0:8]
        send(ss.at[core], ss.at[core], ss_s, ss_r, sibling)

    def finish_spots():
        lane_id = lax.broadcasted_iota(jnp.int32, (1, rows), 1)
        first_lane = lane_id < slide_rows
        lane_position = place * slide_rows + jnp.where(first_lane, lane_id, lane_id - slide_rows)
        lane_valid = (lane_position < jnp.where(first_lane, count_ref[0], count_ref[1])).astype(F32)
        arrived(ss.at[1 - core], ss_r)
        spot = ss[0] + ss[1]
        spot_dot, spot_pred, spot_true = spot[0:1], spot[1:2], spot[2:3]
        spot_inv = lax.rsqrt(spot_pred * spot_true + tiny)
        cos_spot = spot_dot * spot_inv
        spot_back = cos_spot * spot_true / (spot_pred * spot_true + tiny)
        kept["cos"] = jnp.sum(lane_valid * cos_spot, axis=1, keepdims=True)
        vectors = [lane_valid * spot_inv, lane_valid * spot_back, lane_valid, jnp.zeros((5, rows), F32)]
        vr[q] = jnp.concatenate(vectors, axis=0)
        sacc[0] = jnp.zeros_like(sacc[0])

    def gradient(truth, guess, by_row, k):
        pieces = []
        for m in range(slides):
            lo, hi = m * slide_rows, (m + 1) * slide_rows
            inverse, back = gv[m : m + 1, turn_cols(k)], gv[2 + m : 3 + m, turn_cols(k)]
            spot_inv, spot_back, spot_valid = by_row[lo:hi, 0:1], by_row[lo:hi, 1:2], by_row[lo:hi, 2:3]
            pieces.append(
                guess[lo:hi] * (spot_valid * back + spot_back) - truth[lo:hi] * (spot_valid * inverse + spot_inv)
            )
        return jnp.concatenate(pieces, axis=0)

    def head_gradient():
        for p in mates:
            arrived(t0.at[p], t0_r.at[p])
            arrived(p0.at[p], p0_r.at[p])
            arrived(vr.at[p], vr_r.at[p])
        for p in range(PLANE):
            ds[0][share(p), :] = gradient(t0[p], p0[p], vr[p].T, 0)
        sacc[0] += lane_groups(ds[0][share(q), :] * p0[q])

    def send_grad(k):
        if k == 0:
            for p in mates:
                send(vr.at[q], vr.at[q], vr_s, vr_r.at[q], mate(p))
            kept["by_row"] = vr[q].T
            return
        grad = gradient(tg[:, turn_cols(k)], pr[:, turn_cols(k)], kept["by_row"], k)
        here = ds[k].at[share(q)]
        here[...] = grad
        for p in mates:
            send(here, here, d_s.at[k], d_r.at[k, q], mate(p))
        sacc[0] += lane_groups(grad * pr[:, turn_cols(k)])

    def send_terms():
        mass_total, cell_total = kept["mass"], kept["cells"]
        portion = kcell / cell_total
        kl_rows = portion * (jnp.log(counted) - jnp.log(cell_total) - jnp.log(mass) + jnp.log(mass_total))
        dmass = scale_count * valid * (1.0 / mass_total - portion / mass)
        terms = jnp.sum(scale_count * kl_rows, axis=0, keepdims=True) - kept["cos"]
        l1[q] = jnp.broadcast_to(terms, (8, LANES))
        for p in mates:
            send(l1.at[q], l1.at[q], l1_s, l1_r.at[q], mate(p))
        inner = jnp.sum(sacc[0], axis=1, keepdims=True)
        inn[core] = jnp.where(wide == 0, inner, kept["genes", 0] + kept["genes", 1])
        send(inn.at[core], inn.at[core], in_s, in_r, sibling)
        rowv[1] = jnp.broadcast_to(dmass, (rows, LANES))

    middle = lines // 2

    def backward_product(k):
        if k == 0:
            head_gradient()
        else:
            for p in mates:
                arrived(ds[k].at[share(p)], d_r.at[k, p])
        width, spots = backward_widths[k], PLANE * rows

        def lay(at):
            value = ds[k][at, :]
            lay_factor(at, spots, width, value)
            grad_3[at, three_turn_cols(k)] = threefold(value)

        in_blocks(0, spots, lay)
        if not halved(k):

            @pl.loop(0, quarter // TALL)
            def _(step):
                tall = pl.ds(pl.multiple_of(step * TALL, TALL), TALL)
                es[k][tall, :] = product(turned_3[tall, :], factor[0 : 3 * spots, 0:width], ((1,), (0,)))

        for turn in range(2):
            if halved(k):
                side = (1 - z // middle) if turn == 0 else z // middle
                pair = pl.ds(pl.multiple_of(side * middle * cb, middle * cb), middle * cb)
                es[k][pair, :] = product(turned_3[pair, :], factor[0 : 3 * spots, 0:width], ((1,), (0,)))

            @pl.when(z == 0)
            def _():
                if halved(k):
                    pass_up(k, middle if turn == 0 else 1, middle if turn == 0 else middle - 1, turn)
                elif whole(k):
                    if turn == 0:
                        pass_up(k, 1, last, 0)
                elif turn == 0:
                    for line in range(last, 0, -1):
                        pass_up(k, line, 1, line)

            @pl.when(z == last)
            def _():
                if halved(k):
                    pass_down(k, 0 if turn == 0 else middle, middle if turn == 0 else middle - 1, turn)
                elif whole(k):
                    if turn == 0:
                        pass_down(k, 0, last, 0)
                elif turn == 0:
                    for line in range(last):
                        pass_down(k, line, 1, line)

    def halved(k):
        return k == 0

    def whole(k):
        return 0 < k < turns - SPLIT

    def pass_up(k, line, count, slot):
        here = pl.ds(line * cb, count * cb)
        send(es[k].at[here], ru[k].at[here], ru_s.at[k], ru_r.at[k, slot], up)

    def pass_down(k, line, count, slot):
        here = pl.ds(line * cb, count * cb)
        send(es[k].at[here], rd[k].at[here], rd_s.at[k], rd_r.at[k, slot], down)

    def take_up(k, line, count, slot):
        arrived(ru[k].at[pl.ds(line * cb, count * cb)], ru_r.at[k, slot])

    def take_down(k, line, count, slot):
        arrived(rd[k].at[pl.ds(line * cb, count * cb)], rd_r.at[k, slot])

    def add_up(k, line, count):
        def add(at):
            es[k][at, :] += ru[k][at, :]

        in_blocks(line * cb, count * cb, add)

    def add_down(k, line, count):
        def add(at):
            es[k][at, :] += rd[k][at, :]

        in_blocks(line * cb, count * cb, add)

    def rising(k, at):
        if halved(k) or whole(k):
            start = middle if halved(k) else at
            take_up(k, start, lines - start, 0)
            above = max(at + 1, start)
            add_up(k, above, lines - above)
            pass_up(k, above, lines - above, 0)
        else:
            for line in range(last, at, -1):
                take_up(k, line, 1, line)
                add_up(k, line, 1)
                pass_up(k, line, 1, line)

    def falling(k, at):
        if halved(k) or whole(k):
            end = middle if halved(k) else at + 1
            take_down(k, 0, end, 0)
            below = min(at, end)
            add_down(k, 0, below)
            pass_down(k, 0, below, 0)
        else:
            for line in range(at):
                take_down(k, line, 1, line)
                add_down(k, line, 1)
                pass_down(k, line, 1, line)

    def add_near(k):
        for at in range(1, last):

            @pl.when(z == at)
            def _():
                (rising if low(at) else falling)(k, at)

    def add_far(k):
        for at in range(1, last):

            @pl.when(z == at)
            def _():
                (falling if low(at) else rising)(k, at)

    def finish_expr(k):
        for at in range(lines):

            @pl.when(z == at)
            def _():
                if at > 0:
                    if halved(k) and at < middle:
                        take_up(k, at, 1, 1)
                    elif at == last and (halved(k) or whole(k)):
                        take_up(k, at, 1, 0)
                    elif not halved(k) and not whole(k):
                        take_up(k, at, 1, at)
                if at < last:
                    if halved(k) and at >= middle:
                        take_down(k, at, 1, 1)
                    elif at == 0 and (halved(k) or whole(k)):
                        take_down(k, at, 1, 0)
                    elif not halved(k) and not whole(k):
                        take_down(k, at, 1, at)

        from_low, from_high = z > 0, z < last

        @pl.loop(0, cb // BLOCK)
        def _(step):
            here = pl.ds(pl.multiple_of(step * BLOCK, BLOCK), BLOCK)
            own = pl.ds(pl.multiple_of(z * cb + step * BLOCK, BLOCK), BLOCK)
            total = es[k][own, :]
            total = total + jnp.where(from_low, ru[k][own, :], 0.0)
            ge[here, turn_cols(k)] = total + jnp.where(from_high, rd[k][own, :], 0.0)

    def probs_gradient(k):
        at = three_turn_cols(k)

        @pl.loop(0, PLANE * rows // TALL)
        def _(step):
            tall = pl.ds(pl.multiple_of(step * TALL, TALL), TALL)
            part = product(grad_3[tall, at], expr_3[:, at], ((1,), (1,)))
            if k == 0:
                fs[tall, :] = part
            else:
                fs[tall, :] += part

    def slide_of(p, m):
        return pl.ds(pl.multiple_of(p * rows + m * slide_rows, slide_rows), slide_rows)

    def sum_probs_cores():
        for p in mates + (q,):
            fx[p] = fs[slide_of(p, 1 - core), :]
            send(fx.at[p], fy.at[p], fx_s, fx_r.at[p], sibling)

    def return_probs():
        for p in mates:
            arrived(fy.at[p], fx_r.at[p])
            fz[p] = fs[slide_of(p, core), :] + fy[p]
            send(fz.at[p], fr.at[q], f_s, f_r.at[q], mate(p))
        arrived(fy.at[q], fx_r.at[q])
        fr[q] = fs[slide_of(q, core), :] + fy[q]

    def pass_terms():
        for p in mates:
            arrived(l1.at[p], l1_r.at[p])
        l2[z] = (l1[0] + l1[1]) + (l1[2] + l1[3])
        for o in others:
            send(l2.at[z], l2.at[z], l2_s, l2_r.at[z], (o * PLANE + q, core))

    def part_of(slide, m):
        start = slide * slide_rows + m * (slide_rows // 2)
        return pl.ds(pl.multiple_of(start, slide_rows // 2), slide_rows // 2)

    def finish_logits():
        arrived(inn.at[1 - core], in_r)
        rowv[2] = (inn[0] + inn[1]) + rowv[1] * rowv[0]
        for p in mates:
            arrived(fr.at[p], f_r.at[p])
        for m in range(2):

            @pl.loop(0, slide_rows // STEP_ROWS // 2)
            def _(step):
                row_at = (m * (slide_rows // STEP_ROWS // 2) + step) * STEP_ROWS
                at = pl.ds(pl.multiple_of(row_at, STEP_ROWS), STEP_ROWS)
                whole_at = pl.ds(pl.multiple_of(core * slide_rows + row_at, STEP_ROWS), STEP_ROWS)
                by_mass, total_inner = rowv[1, whole_at, 0:1], rowv[2, whole_at, 0:1]
                for p in range(PLANE):
                    for line in range(lines):
                        here, there = pl.ds(line * cb, cb), (line * PLANE + p) * cb
                        grad = fr[p, at, here] + by_mass * weights[:, there : there + cb]
                        glog[whole_at, pl.ds(there, cb)] = pq[p, whole_at, here] * (grad - total_inner)

            here = part_of(core, m)
            send(glog.at[here], glog.at[here], go_s, go_r.at[m], sibling)

    def forward_left():
        for k in range(chunks):

            @pl.when(z < last)
            def _():
                sent(bb[k].at[block(z)], ou_s.at[k])

            @pl.when(z > 0)
            def _():
                sent(bb[k].at[block(z)], od_s.at[k])

            for at in range(1, last):

                @pl.when(z == at)
                def _():
                    sent(bb[k].at[pl.ds(0, at * cb)], fu_s.at[k])
                    sent(bb[k].at[pl.ds((at + 1) * cb, (last - at) * cb)], fd_s.at[k])

        three = pl.ds(0, len(mates))
        sent(ab.at[three, half(0)], a_s)
        sent(ab.at[three, half(0)], a2_s)
        sent(rs.at[three], r_s)
        sent(t0.at[three], t0_s)
        sent(p0.at[three], p0_s)
        for k in range(chunks):
            sent(cr[k].at[three], c_s.at[k])
        sent(s1.at[three], s1_s)
        sent(s2.at[pl.ds(0, last)], s2_s)
        sent(ss.at[0], ss_s)

    steps = {
        "far": forward_far,
        "near": forward_near,
        "share": share_logits,
        "take": take_probs,
        "whole": gathered,
        "product": forward_product,
        "sum": finish_pred,
        "turn": transpose,
        "plane": sum_plane,
        "line": sum_line,
        "genes": finish_genes,
        "cores": sum_cores,
        "spots": finish_spots,
        "grad": send_grad,
        "terms": send_terms,
        "backward": backward_product,
        "probs": probs_gradient,
        "exchange": sum_probs_cores,
        "return": return_probs,
        "loss": pass_terms,
        "logits": finish_logits,
        "add_near": add_near,
        "add_far": add_far,
        "expr": finish_expr,
        "left": forward_left,
    }
    for name, *where in STEPS:
        steps[name](*where)

    for o in others:
        arrived(l2.at[o], l2_r.at[o])
    loss = l2[0]
    for line in range(1, lines):
        loss = loss + l2[line]
    loss_ref[...] = loss[0:1, 0:1] - (inn[0, 0:1, 1:2] + inn[1, 0:1, 1:2])
    for m in range(2):
        arrived(glog.at[part_of(1 - core, m)], go_r.at[m])

    for k in range(turns):
        for at in range(lines):

            @pl.when(z == at)
            def _():
                if at < last:
                    sent(es[k].at[pl.ds((at + 1) * cb, (last - at) * cb)], ru_s.at[k])
                if at > 0:
                    sent(es[k].at[pl.ds(0, at * cb)], rd_s.at[k])

    three = pl.ds(0, len(mates))
    for k in range(1, turns):
        sent(ds[k].at[pl.ds(0, len(mates) * rows)], d_s.at[k])
    sent(vr.at[three], vr_s)
    sent(inn.at[0], in_s)
    sent(l1.at[three], l1_s)
    sent(l2.at[pl.ds(0, last)], l2_s)
    sent(fr.at[three], f_s)
    sent(fx, fx_s)
    sent(glog.at[half(0)], go_s)


def lane_groups(value):
    parts = [value[:, at : at + LANES] for at in range(0, value.shape[1], LANES)]
    return functools.reduce(lambda a, b: a + b, parts)


def grouped(refs, sizes):
    at = 0
    for size in sizes:
        yield refs[at : at + size]
        at += size


def deliver(pred_in, loss_in, glog_in, gexp_in, pred_ref, loss_ref, glog_ref, gexp_ref, sems):
    slides, slide_rows = pred_ref.shape[0], pred_ref.shape[1]
    pairs = [(gexp_in, gexp_ref), (loss_in, loss_ref)]
    for m in range(slides):
        part = pl.ds(m * slide_rows, slide_rows)
        pairs += [(glog_in.at[part], glog_ref.at[m]), (pred_in.at[part], pred_ref.at[m])]
    copies = [pltpu.make_async_copy(src, dst, sems.at[at]) for at, (src, dst) in enumerate(pairs)]
    for copy in copies:
        copy.start()
    for copy in copies:
        copy.wait()


def plane_call(logits, expr, spatial, slide_spots, spot_cells, cell_prior, lines):
    slides, slide_rows, cells = logits.shape
    rows = slides * slide_rows
    cb, genes = expr.shape
    quarter = lines * cb
    spots = PLANE * rows
    chunks, turns = len(FORWARD), len(BACKWARD)
    dma = pltpu.SemaphoreType.DMA
    vmem = pltpu.VMEM
    anywhere = pl.BlockSpec(memory_space=pl.ANY)
    in_vmem = pl.BlockSpec(memory_space=pltpu.VMEM)
    scratch = [
        pltpu.SMEM((slides,), jnp.int32),
        vmem((slides, slide_rows), jnp.int32),
        vmem((1, cells), jnp.int32),
        vmem((rows, cells), F32),
        vmem((PLANE, slide_rows, quarter), F32),
        vmem((rows, genes), F32),
        vmem((cb, genes), F32),
        vmem((PLANE, rows, quarter), F32),
        vmem((PLANE, rows, quarter), F32),
        vmem((PLANE, rows, quarter), F32),
        vmem((spots, 3 * quarter), BF16),
        vmem((quarter, 3 * spots), BF16),
        vmem((quarter, 3 * genes), BF16),
        vmem((3, rows, LANES), F32),
        vmem((PLANE, 8, genes), F32),
        vmem((lines, 8, genes), F32),
        vmem((8, genes), F32),
        vmem((2, 8, rows), F32),
        vmem((3, rows, LANES), F32),
        vmem((PLANE, 8, rows), F32),
        vmem((spots, 3 * genes), BF16),
        vmem((3 * max(quarter, spots), max(FORWARD + BACKWARD)), BF16),
        vmem((PLANE, rows, BACKWARD[0]), F32),
        vmem((PLANE, rows, BACKWARD[0]), F32),
        vmem((PLANE, 8, rows), F32),
        vmem((spots, quarter), F32),
        vmem((PLANE, slide_rows, quarter), F32),
        vmem((PLANE, slide_rows, quarter), F32),
        vmem((PLANE, slide_rows, quarter), F32),
        vmem((PLANE, slide_rows, quarter), F32),
        vmem((2, rows, LANES), F32),
        vmem((PLANE, 8, LANES), F32),
        vmem((lines, 8, LANES), F32),
        dma((2 * slides + 4,)),
        dma((chunks,)),
        dma((chunks,)),
        dma((chunks,)),
        dma((chunks,)),
        dma((chunks,)),
        dma((chunks,)),
        dma((chunks,)),
        dma((chunks,)),
        dma,
        dma((PLANE,)),
        dma,
        dma((PLANE,)),
        dma,
        dma((PLANE,)),
        dma((chunks,)),
        dma((chunks, PLANE)),
        dma,
        dma((2, PLANE)),
        dma,
        dma((2, lines)),
        dma,
        dma,
        dma((turns,)),
        dma((turns, PLANE)),
        dma((turns,)),
        dma((turns, lines)),
        dma((turns,)),
        dma((turns, lines)),
        dma,
        dma((PLANE,)),
        dma,
        dma((PLANE,)),
        dma,
        dma((2,)),
        dma,
        dma,
        dma,
        dma((PLANE,)),
        dma,
        dma((lines,)),
        dma,
        dma((PLANE,)),
        dma,
        dma((PLANE,)),
        dma,
        dma((PLANE,)),
    ]
    for shape, widths in (
        ((quarter,), FORWARD),
        ((spots,), FORWARD),
        ((PLANE, rows), FORWARD),
        ((spots,), BACKWARD),
        ((quarter,), BACKWARD),
        ((quarter,), BACKWARD),
        ((quarter,), BACKWARD),
    ):
        scratch += [vmem(shape + (width,), F32) for width in widths]
    in_hbm = functools.partial(pltpu.with_memory_space_constraint, memory_space=pltpu.HBM)
    in_place = functools.partial(pltpu.with_memory_space_constraint, memory_space=pltpu.VMEM)
    results = pl.pallas_call(
        functools.partial(plane_kernel, lines, FORWARD, BACKWARD),
        out_shape=(
            vmem((rows, genes), F32),
            vmem((1, 1), F32),
            vmem((rows, cells), F32),
            vmem((cb, genes), F32),
        ),
        in_specs=[anywhere] * 6,
        out_specs=(in_vmem,) * 4,
        scratch_shapes=scratch,
        compiler_params=pltpu.CompilerParams(
            collective_id=0, has_side_effects=True, vmem_limit_bytes=48 * 1024 * 1024
        ),
    )(*map(in_hbm, (logits, expr, spatial, slide_spots, spot_cells, cell_prior.reshape(1, cells))))
    pred, loss, grad_logits, grad_expr = pl.pallas_call(
        deliver,
        out_shape=(
            jax.ShapeDtypeStruct((slides, slide_rows, genes), F32),
            jax.ShapeDtypeStruct((1, 1), F32),
            jax.ShapeDtypeStruct((slides, slide_rows, cells), F32),
            jax.ShapeDtypeStruct((cb, genes), F32),
        ),
        in_specs=[anywhere] * 4,
        out_specs=(anywhere,) * 4,
        scratch_shapes=[dma((2 * slides + 2,))],
        compiler_params=pltpu.CompilerParams(vmem_limit_bytes=4 * 1024 * 1024),
    )(*map(in_place, results))
    return pred, loss.reshape(()), grad_logits, grad_expr


def general_plan(logits, expr, spatial, slide_spots, spot_cells, cell_prior):
    place = lax.axis_index("spot")
    side = lax.axis_index("gene")
    rows_all = logits.shape[1]
    cell_rows = expr.shape[0]
    weights = cell_prior.astype(jnp.float32) / fixed_point
    gene_share = (place == 0).astype(jnp.float32)
    row_share = (side == 0).astype(jnp.float32)
    own_weights = lax.dynamic_slice_in_dim(weights, place * cell_rows, cell_rows, 0)
    expr_acc = jnp.zeros((cell_rows, expr.shape[1]), jnp.float32)
    loss_local = jnp.zeros((), jnp.float32)
    pred_list = []
    grad_list = []
    for slide in range(logits.shape[0]):
        logit_rows = logits[slide]
        counted = spot_cells[slide].astype(jnp.float32)
        target = spatial[slide]
        positions = place * rows_all + jnp.arange(rows_all, dtype=jnp.int32)
        valid = (positions < slide_spots[slide]).astype(jnp.float32)
        peak = jnp.max(logit_rows, axis=1, keepdims=True)
        raised = jnp.exp(logit_rows - peak)
        probs = raised / jnp.sum(raised, axis=1, keepdims=True)
        mass = jnp.dot(probs, weights, precision=lax.Precision.HIGHEST)
        blocks = lax.all_to_all(probs, "spot", split_axis=1, concat_axis=0, tiled=True)
        pred = lax.psum_scatter(
            jnp.dot(blocks, expr, precision=lax.Precision.HIGHEST),
            "spot",
            scatter_dimension=0,
            tiled=True,
        )
        gene_dot = jnp.sum(valid[:, None] * pred * target, axis=0)
        gene_pred = jnp.sum(valid[:, None] * pred * pred, axis=0)
        gene_true = jnp.sum(valid[:, None] * target * target, axis=0)
        mass_part = jnp.sum(valid * mass)
        kcell = valid * counted
        cell_part = jnp.sum(kcell)
        spot_dot = jnp.sum(pred * target, axis=1)
        spot_pred = jnp.sum(pred * pred, axis=1)
        spot_true = jnp.sum(target * target, axis=1)
        gene_dot, gene_pred, gene_true, mass_total, cell_total = lax.psum(
            (gene_dot, gene_pred, gene_true, mass_part, cell_part), "spot"
        )
        spot_dot, spot_pred, spot_true = lax.psum((spot_dot, spot_pred, spot_true), "gene")
        gene_inv = lax.rsqrt(gene_pred * gene_true + tiny)
        cos_gene = gene_dot * gene_inv
        spot_inv = lax.rsqrt(spot_pred * spot_true + tiny)
        cos_spot = spot_dot * spot_inv
        share = kcell / cell_total
        scale_count = slide_spots[slide].astype(jnp.float32)
        kl_part = jnp.sum(
            share * (jnp.log(counted) - jnp.log(cell_total) - jnp.log(mass) + jnp.log(mass_total))
        )
        loss_local = loss_local - gene_share * jnp.sum(cos_gene)
        loss_local = loss_local + row_share * (scale_count * kl_part - jnp.sum(valid * cos_spot))
        gene_back = cos_gene * gene_true / (gene_pred * gene_true + tiny)
        spot_back = cos_spot * spot_true / (spot_pred * spot_true + tiny)
        dpred = -valid[:, None] * (
            target * (gene_inv[None, :] + spot_inv[:, None])
            - pred * gene_back[None, :]
            - pred * spot_back[:, None]
        )
        dmass = scale_count * valid * (1.0 / mass_total - share / mass)
        pred_list.append(pred)
        grads_full, mass_full = (
            lax.all_gather(dpred, "spot", axis=0, tiled=True),
            lax.all_gather(dmass, "spot", axis=0, tiled=True),
        )
        dprob_cells = jnp.dot(grads_full, expr.T, precision=lax.Precision.HIGHEST)
        dprob_cells = lax.psum(dprob_cells, "gene")
        expr_acc = expr_acc + lax.dot_general(
            blocks, grads_full, (((0,), (0,)), ((), ())), precision=lax.Precision.HIGHEST
        )
        dprob_cells = dprob_cells + mass_full[:, None] * own_weights[None, :]
        dprob_rows = lax.all_to_all(dprob_cells, "spot", split_axis=0, concat_axis=1, tiled=True)
        inner = jnp.sum(probs * dprob_rows, axis=1, keepdims=True)
        dlogit = probs * (dprob_rows - inner)
        grad_list.append(dlogit)
    loss = lax.psum(loss_local, ("spot", "gene"))
    return (jnp.stack(pred_list), loss, jnp.stack(grad_list), expr_acc)


def solution(mesh):
    places = mesh.shape["spot"]

    def on_device(logits, expr, spatial, slide_spots, spot_cells, cell_prior):
        if places == PLANE * PLANE and mesh.shape["gene"] == 2 and expr.shape[1] == sum(FORWARD):
            return plane_call(
                logits, expr, spatial, slide_spots, spot_cells, cell_prior, places // PLANE
            )
        return general_plan(logits, expr, spatial, slide_spots, spot_cells, cell_prior)

    in_specs = (
        P(None, "spot", None),
        P("spot", "gene"),
        P(None, "spot", "gene"),
        P(),
        P(None, "spot"),
        P(),
    )
    out_specs = (P(None, "spot", "gene"), P(), P(None, "spot", None), P("spot", "gene"))
    return jax.shard_map(
        on_device, mesh=mesh, in_specs=in_specs, out_specs=out_specs, check_vma=False
    )
```

```python
import functools

import jax
import jax.numpy as jnp
from jax import lax
from jax.experimental import pallas as pl
from jax.experimental.pallas import tpu as pltpu
from jax.sharding import PartitionSpec as P

tiny = 1e-06
fixed_point = 16384.0
F32 = jnp.float32
BF16 = jnp.bfloat16
MESH = pl.DeviceIdType.MESH

PLANE = 4
LANES = 128
STEP_ROWS = 16
BLOCK = 32
TALL = 256
FORWARD = (128, 256, 256, 256, 128)
BACKWARD = (128, 128, 256, 256, 256)
SPLIT = 2
LEAD = 2
NEAR_LEAD = 3
EARLY = 3
LATE = (2, 3, 4)
STEPS = (
    ("far", 0),
    ("far", 1),
    ("near", 0),
    ("share",),
    ("far", 2),
    ("far", 3),
    ("take",),
    ("whole", 0),
    ("near", 1),
    ("product", 0),
    ("sum", 0),
    ("whole", 1),
    ("near", 2),
    ("product", 1),
    ("whole", 2),
    ("product", 2),
    ("whole", 3),
    ("near", 3),
    ("product", 3),
    ("whole", 4),
    ("far", 4),
    ("near", 4),
    ("product", 4),
    ("turn", 0),
    ("sum", 1),
    ("sum", 2),
    ("plane", 0),
    ("turn", 1),
    ("sum", 3),
    ("line", 0),
    ("sum", 4),
    ("plane", 1),
    ("cores",),
    ("genes", 0),
    ("spots",),
    ("grad", 0),
    ("grad", 1),
    ("grad", 2),
    ("line", 1),
    ("backward", 0),
    ("late", 2),
    ("backward", 1),
    ("add_near", 0),
    ("genes", 1),
    ("grad", 3),
    ("backward", 2),
    ("late", 3),
    ("probs", 0),
    ("add_far", 0),
    ("probs", 1),
    ("expr", 0),
    ("grad", 4),
    ("add_near", 1),
    ("probs", 2),
    ("terms",),
    ("late", 4),
    ("backward", 3),
    ("probs", 3),
    ("add_near", 2),
    ("backward", 4),
    ("add_far", 1),
    ("probs", 4),
    ("exchange",),
    ("add_near", 3),
    ("add_far", 2),
    ("left",),
    ("return",),
    ("loss",),
    ("add_far", 3),
    ("expr", 1),
    ("add_near", 4),
    ("logits",),
    ("add_far", 4),
    ("expr", 2),
    ("expr", 3),
    ("expr", 4),
)


def halves(value):
    high = value.astype(BF16)
    return high, (value - high.astype(F32)).astype(BF16)


def threefold(value):
    high, low = halves(value)
    return jnp.concatenate([high, high, low], axis=1)


def product(a, b, contract):
    return lax.dot_general(a, b, (contract, ((), ())), preferred_element_type=F32)


def plane_kernel(lines, forward_widths, backward_widths, *refs):
    chunks, turns = len(forward_widths), len(backward_widths)
    (
        (logits_ref, expr_ref, spatial_ref, count_in, cells_in, prior_in),
        (pr, loss_ref, glog, ge),
        (count_ref, cells_ref, prior_ref, lg, lq, tg, ex, pq, ab, af, probs_3, turned_3, expr_3, sacc, s1, s2, gv, ss, rowv, rs),
        (grad_3, factor, t0, p0, vr, fs, fx, fy, fz, fr, inn, l1, l2),
        (loc, ou_s, ou_r, od_s, od_r, fu_s, fu_r, fd_s, fd_r, a_s, a_r, a2_s, a2_r, r_s, r_r),
        (c_s, c_r, s1_s, s1_r, s2_s, s2_r, ss_s, ss_r, d_s, d_r, ru_s, ru_r, rd_s, rd_r),
        (f_s, f_r, fx_s, fx_r, go_s, go_r, in_s, in_r, l1_s, l1_r, l2_s, l2_r, t0_s, t0_r, p0_s, p0_r, vr_s, vr_r),
        bb,
        cs,
        cr,
        ds,
        es,
        ru,
        rd,
    ) = grouped(refs, (6, 4, 20, 13, 15, 14, 18, chunks, chunks, chunks, turns, turns, turns, turns))
    place = lax.axis_index("spot")
    core = lax.axis_index("gene")
    z = place // PLANE
    q = place % PLANE
    col, row = q % 2, q // 2
    mates = ((1 - row) * 2 + 1 - col, row * 2 + 1 - col, (1 - row) * 2 + col)
    others = tuple((z + step) % lines for step in range(1, lines))
    up, down = (place + PLANE, core), (place - PLANE, core)
    sibling = (place, 1 - core)
    slides, slide_rows = logits_ref.shape[0], logits_ref.shape[1]
    rows = slides * slide_rows
    cb = expr_ref.shape[0]
    genes = expr_ref.shape[1]
    last = lines - 1

    def mate(p):
        return (z * PLANE + p, core)

    def send(src, dst, send_sem, recv_sem, device):
        copy = pltpu.make_async_remote_copy(
            src_ref=src, dst_ref=dst, send_sem=send_sem, recv_sem=recv_sem, device_id=device, device_id_type=MESH
        )
        copy.start()

    def arrived(dst, recv_sem):
        pltpu.make_async_copy(dst, dst, recv_sem).wait()

    sent = arrived

    def cols(k):
        return pl.ds(sum(forward_widths[:k]), forward_widths[k])

    def turn_cols(k):
        return pl.ds(sum(backward_widths[:k]), backward_widths[k])

    def block(index):
        return pl.ds(pl.multiple_of(index * cb, cb), cb)

    def share(index):
        return pl.ds(pl.multiple_of(index * rows, rows), rows)

    def half(index):
        return pl.ds(pl.multiple_of(index * slide_rows, slide_rows), slide_rows)

    small = ((prior_in, prior_ref), (count_in, count_ref), (cells_in, cells_ref))
    pltpu.make_async_copy(expr_ref, ex, loc.at[2 * slides]).start()
    for m in range(slides):
        pltpu.make_async_copy(logits_ref.at[m], lg.at[half(m)], loc.at[m]).start()
    for at, (src, dst) in enumerate(small):
        pltpu.make_async_copy(src, dst, loc.at[2 * slides + 1 + at]).start()
    for m in range(slides):
        pltpu.make_async_copy(spatial_ref.at[m], tg.at[half(m)], loc.at[slides + m]).start()

    barrier = pltpu.get_barrier_semaphore()
    for p in mates:
        pl.semaphore_signal(barrier, inc=1, device_id=mate(p), device_id_type=MESH)
    for o in others:
        pl.semaphore_signal(barrier, inc=1, device_id=(o * PLANE + q, core), device_id_type=MESH)
    pl.semaphore_signal(barrier, inc=1, device_id=sibling, device_id_type=MESH)
    pltpu.make_async_copy(expr_ref, ex, loc.at[2 * slides]).wait()
    for k in range(chunks):
        bb[k][block(z), :] = ex[:, cols(k)]
    for m in range(slides):
        pltpu.make_async_copy(logits_ref.at[m], lg.at[half(m)], loc.at[m]).wait()
    for p in range(PLANE):
        for line in range(lines):
            lq[p, :, pl.ds(line * cb, cb)] = lg[half(core), pl.ds((line * PLANE + p) * cb, cb)]
    pl.semaphore_wait(barrier, len(mates) + len(others) + 1)

    def own_up(k):
        here = bb[k].at[block(z)]
        send(here, here, ou_s.at[k], ou_r.at[k], up)

    def own_down(k):
        here = bb[k].at[block(z)]
        send(here, here, od_s.at[k], od_r.at[k], down)

    def low(at):
        return 2 * at < lines

    for at in range(lines):

        @pl.when(z == at)
        def _():
            for k in range(chunks):
                if at < last and (at == 0 or k < (LEAD if low(at) else NEAR_LEAD)):
                    own_up(k)
                if at > 0 and (at == last or k < (NEAR_LEAD if low(at) else LEAD)):
                    own_down(k)

    for p in mates:
        send(lq.at[p], ab.at[q, half(core)], a_s, a_r.at[q], mate(p))

    def from_below(k, at):
        arrived(bb[k].at[pl.ds((at - 1) * cb, cb)], ou_r.at[k])
        if at > 1:
            arrived(bb[k].at[pl.ds(0, (at - 1) * cb)], fu_r.at[k])

    def from_above(k, at):
        arrived(bb[k].at[pl.ds((at + 1) * cb, cb)], od_r.at[k])
        if at < last - 1:
            arrived(bb[k].at[pl.ds((at + 2) * cb, (last - 1 - at) * cb)], fd_r.at[k])

    def upward(k, at):
        from_below(k, at)
        here = bb[k].at[pl.ds(0, at * cb)]
        send(here, here, fu_s.at[k], fu_r.at[k], up)

    def downward(k, at):
        from_above(k, at)
        here = bb[k].at[pl.ds((at + 1) * cb, (last - at) * cb)]
        send(here, here, fd_s.at[k], fd_r.at[k], down)

    def forward_far(k):
        for at in range(1, last):

            @pl.when(z == at)
            def _():
                (upward if low(at) else downward)(k, at)
                if k + LEAD < chunks:
                    (own_up if low(at) else own_down)(k + LEAD)

    def forward_near(k):
        for at in range(1, last):

            @pl.when(z == at)
            def _():
                (downward if low(at) else upward)(k, at)
                if k + NEAR_LEAD < chunks:
                    (own_down if low(at) else own_up)(k + NEAR_LEAD)

    def gathered(k):
        @pl.when(z == 0)
        def _():
            from_above(k, 0)

        @pl.when(z == last)
        def _():
            from_below(k, last)

    for at, (src, dst) in enumerate(small):
        pltpu.make_async_copy(src, dst, loc.at[2 * slides + 1 + at]).wait()
    weights = prior_ref[...].astype(F32) / fixed_point

    @pl.loop(0, rows // STEP_ROWS)
    def _(step):
        at = pl.ds(pl.multiple_of(step * STEP_ROWS, STEP_ROWS), STEP_ROWS)
        value = lg[at, :]
        peak = jnp.max(value, axis=1, keepdims=True)
        raised = jnp.exp(value - peak)
        scale = 1.0 / jnp.sum(raised, axis=1, keepdims=True)
        probs = raised * scale
        mass_rows = jnp.sum(probs * weights, axis=1, keepdims=True)
        rowv[0, at, :] = jnp.broadcast_to(mass_rows, (STEP_ROWS, LANES))
        rowv[1, at, :] = jnp.broadcast_to(peak, (STEP_ROWS, LANES))
        rowv[2, at, :] = jnp.broadcast_to(scale, (STEP_ROWS, LANES))
        for p in range(PLANE):
            for line in range(lines):
                at_cells = (line * PLANE + p) * cb
                pq[p, at, pl.ds(line * cb, cb)] = probs[:, at_cells : at_cells + cb]

    wide = lax.broadcasted_iota(jnp.int32, (rows, LANES), 1)
    rs[q] = jnp.where(wide == 0, rowv[1], rowv[2]).T[0:8]
    for p in mates:
        send(rs.at[q], rs.at[q], r_s, r_r.at[q], mate(p))

    rid = lax.broadcasted_iota(jnp.int32, (rows, 1), 0)
    first = rid < slide_rows
    position = place * slide_rows + jnp.where(first, rid, rid - slide_rows)
    count = jnp.where(first, count_ref[0], count_ref[1])
    valid = (position < count).astype(F32)
    scale_count = count.astype(F32)
    square = (slide_rows, slide_rows)
    eye = lax.broadcasted_iota(jnp.int32, square, 0) == lax.broadcasted_iota(jnp.int32, square, 1)
    counted = jnp.concatenate(
        [
            jnp.sum(jnp.where(eye, cells_ref[m : m + 1, :].astype(F32), 0.0), axis=1, keepdims=True)
            for m in range(slides)
        ],
        axis=0,
    )
    mass = rowv[0, :, 0:1]
    kcell = valid * counted

    def by_slide(value):
        return [jnp.sum(value[m * slide_rows : (m + 1) * slide_rows], axis=0, keepdims=True) for m in range(slides)]

    mass_parts = by_slide(valid * mass)
    cell_parts = by_slide(kcell)
    lane = lax.broadcasted_iota(jnp.int32, (1, LANES), 1)
    scalars = jnp.zeros((1, LANES), F32)
    for at, value in enumerate(mass_parts + cell_parts):
        scalars = jnp.where(lane == at, value, scalars)
    for m in range(slides):
        pltpu.make_async_copy(spatial_ref.at[m], tg.at[half(m)], loc.at[slides + m]).wait()

    head = backward_widths[0]
    t0[q] = tg[:, 0:head]
    for p in mates:
        send(t0.at[q], t0.at[q], t0_s, t0_r.at[q], mate(p))
    sacc[...] = jnp.zeros_like(sacc)
    s1[q, 3 * slides :, :] = jnp.zeros((8 - 3 * slides, genes), F32)
    s1[q, 3 * slides : 3 * slides + 1, 0:LANES] = scalars

    def share_logits():
        for p in (mates[1], mates[2], mates[0]):
            here = ab.at[p, half(core)]
            arrived(here, a_r.at[p])
            send(here, here, a2_s, a2_r.at[p], sibling)

    def lay_probs(p, at, value):
        af[p, at, :] = value
        there = pl.ds(pl.multiple_of(p * rows + at.start, BLOCK), BLOCK)
        probs_3[there, :] = threefold(value)

    def take_probs():
        in_blocks(0, rows, lambda at: lay_probs(q, at, pq[q, at, :]))
        for p in (mates[1], mates[2], mates[0]):
            arrived(rs.at[p], r_r.at[p])
            arrived(ab.at[p, half(1 - core)], a2_r.at[p])
            rowv[1] = jnp.concatenate([rs[p].T, jnp.zeros((rows, LANES - 8), F32)], axis=1)

            def take(at):
                probs = jnp.exp(ab[p, at, :] - rowv[1, at, 0:1]) * rowv[1, at, 1:2]
                lay_probs(p, at, probs)

            in_blocks(0, rows, take)

    def transpose(part):
        @pl.loop(0, PLANE // 2)
        def _(step):
            p = part * (PLANE // 2) + step
            high, low_part = halves(af[p].T)
            for third, value in enumerate((high, high, low_part)):
                turned_3[:, pl.ds(pl.multiple_of(third * PLANE * rows + p * rows, rows), rows)] = value

    def in_blocks(start, count, body):
        @pl.loop(0, count // BLOCK)
        def _(step):
            body(pl.ds(pl.multiple_of(start + step * BLOCK, BLOCK), BLOCK))

    quarter = lines * cb

    def lay_factor(at, length, width, value):
        high, low_part = halves(value)
        for third, part in enumerate((high, low_part, high)):
            here = pl.ds(pl.multiple_of(third * length + at.start, BLOCK), BLOCK)
            factor[here, 0:width] = part

    def keep_expr(k, at, value):
        start = sum(forward_widths[:k])
        for turn in range(turns):
            origin, width = sum(backward_widths[:turn]), backward_widths[turn]
            lo, hi = max(start, origin), min(start + forward_widths[k], origin + width)
            if lo < hi:
                high, low_part = halves(value[:, lo - start : hi - start])
                for third, part in enumerate((high, low_part, high)):
                    expr_3[at, pl.ds(3 * origin + third * width + lo - origin, hi - lo)] = part

    def three_turn_cols(k):
        return pl.ds(3 * sum(backward_widths[:k]), 3 * backward_widths[k])

    def forward_product(k):
        width = forward_widths[k]

        def lay(at):
            value = bb[k][at, :]
            lay_factor(at, quarter, width, value)
            keep_expr(k, at, value)

        in_blocks(0, quarter, lay)
        if k < chunks - 1:

            @pl.loop(0, PLANE * rows // TALL)
            def _(step):
                tall = pl.ds(pl.multiple_of(step * TALL, TALL), TALL)
                cs[k][tall, :] = product(probs_3[tall, :], factor[0 : 3 * quarter, 0:width], ((1,), (0,)))

            for p in mates:
                pass_pred(k, p)
        else:
            for side, served in ((1 - row, (mates[0], mates[2])), (row, (mates[1],))):
                pair = pl.ds(pl.multiple_of(2 * side * rows, 2 * rows), 2 * rows)
                cs[k][pair, :] = product(probs_3[pair, :], factor[0 : 3 * quarter, 0:width], ((1,), (0,)))
                for p in served:
                    pass_pred(k, p)

    def pass_pred(k, p):
        send(cs[k].at[share(p)], cr[k].at[q], c_s.at[k], c_r.at[k, q], mate(p))

    def finish_pred(k):
        total = cs[k][share(q), :]
        for p in mates:
            arrived(cr[k].at[p], c_r.at[k, p])
            total = total + cr[k][p]
        pr[:, cols(k)] = total
        if k == 0:
            p0[q] = total[:, 0:head]
            for p in mates:
                send(p0.at[q], p0.at[q], p0_s, p0_r.at[q], mate(p))
        truth = tg[:, cols(k)]
        for at, value in enumerate((total * truth, total * total, truth * truth)):
            sacc[at] += lane_groups(value)
        kept = valid * total
        stats = by_slide(kept * truth) + by_slide(kept * total) + by_slide(valid * truth * truth)
        s1[q, 0 : 3 * slides, cols(k)] = jnp.concatenate(stats, axis=0)

    early = sum(forward_widths[:EARLY])
    parts = (pl.ds(0, early), pl.ds(early, genes - early))

    def sum_plane(at):
        for p in mates:
            send(s1.at[q, :, parts[at]], s1.at[q, :, parts[at]], s1_s, s1_r.at[at, q], mate(p))

    def sum_line(at):
        for p in mates:
            arrived(s1.at[p, :, parts[at]], s1_r.at[at, p])
        s2[z, :, parts[at]] = (s1[0, :, parts[at]] + s1[1, :, parts[at]]) + (s1[2, :, parts[at]] + s1[3, :, parts[at]])
        for o in others:
            send(s2.at[z, :, parts[at]], s2.at[z, :, parts[at]], s2_s, s2_r.at[at, z], (o * PLANE + q, core))

    kept = {}

    def finish_genes(at):
        for o in others:
            arrived(s2.at[o, :, parts[at]], s2_r.at[at, o])
        total = s2[0, :, parts[at]]
        for line in range(1, lines):
            total = total + s2[line, :, parts[at]]
        gene_dot, gene_pred, gene_true = total[0:2], total[2:4], total[4:6]
        gene_inv = lax.rsqrt(gene_pred * gene_true + tiny)
        cos_gene = gene_dot * gene_inv
        gv[0:2, parts[at]] = gene_inv
        gv[2:4, parts[at]] = cos_gene * gene_true / (gene_pred * gene_true + tiny)
        kept["genes", at] = jnp.sum(jnp.sum(cos_gene, axis=1, keepdims=True), axis=0, keepdims=True)
        if at == 0:
            kept["mass"] = jnp.where(first, total[6:7, 0:1], total[6:7, 1:2])
            kept["cells"] = jnp.where(first, total[6:7, 2:3], total[6:7, 3:4])

    def sum_cores():
        sums = [jnp.sum(sacc[at], axis=1, keepdims=True) for at in range(3)]
        ss[core] = jnp.where(wide == 0, sums[0], jnp.where(wide == 1, sums[1], sums[2])).T[0:8]
        send(ss.at[core], ss.at[core], ss_s, ss_r, sibling)

    def finish_spots():
        lane_id = lax.broadcasted_iota(jnp.int32, (1, rows), 1)
        first_lane = lane_id < slide_rows
        lane_position = place * slide_rows + jnp.where(first_lane, lane_id, lane_id - slide_rows)
        lane_valid = (lane_position < jnp.where(first_lane, count_ref[0], count_ref[1])).astype(F32)
        arrived(ss.at[1 - core], ss_r)
        spot = ss[0] + ss[1]
        spot_dot, spot_pred, spot_true = spot[0:1], spot[1:2], spot[2:3]
        spot_inv = lax.rsqrt(spot_pred * spot_true + tiny)
        cos_spot = spot_dot * spot_inv
        spot_back = cos_spot * spot_true / (spot_pred * spot_true + tiny)
        kept["cos"] = jnp.sum(lane_valid * cos_spot, axis=1, keepdims=True)
        vectors = [lane_valid * spot_inv, lane_valid * spot_back, lane_valid, jnp.zeros((5, rows), F32)]
        vr[q] = jnp.concatenate(vectors, axis=0)
        sacc[0] = jnp.zeros_like(sacc[0])

    def gradient(truth, guess, by_row, k):
        pieces = []
        for m in range(slides):
            lo, hi = m * slide_rows, (m + 1) * slide_rows
            inverse, back = gv[m : m + 1, turn_cols(k)], gv[2 + m : 3 + m, turn_cols(k)]
            spot_inv, spot_back, spot_valid = by_row[lo:hi, 0:1], by_row[lo:hi, 1:2], by_row[lo:hi, 2:3]
            pieces.append(
                guess[lo:hi] * (spot_valid * back + spot_back) - truth[lo:hi] * (spot_valid * inverse + spot_inv)
            )
        return jnp.concatenate(pieces, axis=0)

    def head_gradient():
        for p in mates:
            arrived(t0.at[p], t0_r.at[p])
            arrived(p0.at[p], p0_r.at[p])
            arrived(vr.at[p], vr_r.at[p])
        for p in range(PLANE):
            ds[0][share(p), :] = gradient(t0[p], p0[p], vr[p].T, 0)
        sacc[0] += lane_groups(ds[0][share(q), :] * p0[q])

    def pass_grad(k):
        here = ds[k].at[share(q)]
        for p in mates:
            send(here, here, d_s.at[k], d_r.at[k, q], mate(p))

    def pass_late(k):
        @pl.when(core == 1)
        def _():
            pass_grad(k)

    def send_grad(k):
        if k == 0:
            for p in mates:
                send(vr.at[q], vr.at[q], vr_s, vr_r.at[q], mate(p))
            kept["by_row"] = vr[q].T
            return
        grad = gradient(tg[:, turn_cols(k)], pr[:, turn_cols(k)], kept["by_row"], k)
        ds[k][share(q), :] = grad
        if k in LATE:

            @pl.when(core == 0)
            def _():
                pass_grad(k)
        else:
            pass_grad(k)
        sacc[0] += lane_groups(grad * pr[:, turn_cols(k)])

    def send_terms():
        mass_total, cell_total = kept["mass"], kept["cells"]
        portion = kcell / cell_total
        kl_rows = portion * (jnp.log(counted) - jnp.log(cell_total) - jnp.log(mass) + jnp.log(mass_total))
        dmass = scale_count * valid * (1.0 / mass_total - portion / mass)
        terms = jnp.sum(scale_count * kl_rows, axis=0, keepdims=True) - kept["cos"]
        l1[q] = jnp.broadcast_to(terms, (8, LANES))
        for p in mates:
            send(l1.at[q], l1.at[q], l1_s, l1_r.at[q], mate(p))
        inner = jnp.sum(sacc[0], axis=1, keepdims=True)
        inn[core] = jnp.where(wide == 0, inner, kept["genes", 0] + kept["genes", 1])
        send(inn.at[core], inn.at[core], in_s, in_r, sibling)
        rowv[1] = jnp.broadcast_to(dmass, (rows, LANES))

    middle = lines // 2

    def backward_product(k):
        if k == 0:
            head_gradient()
        else:
            for p in mates:
                arrived(ds[k].at[share(p)], d_r.at[k, p])
        width, spots = backward_widths[k], PLANE * rows

        def lay(at):
            value = ds[k][at, :]
            lay_factor(at, spots, width, value)
            grad_3[at, three_turn_cols(k)] = threefold(value)

        in_blocks(0, spots, lay)
        if not halved(k):

            @pl.loop(0, quarter // TALL)
            def _(step):
                tall = pl.ds(pl.multiple_of(step * TALL, TALL), TALL)
                es[k][tall, :] = product(turned_3[tall, :], factor[0 : 3 * spots, 0:width], ((1,), (0,)))

        for turn in range(2):
            if halved(k):
                side = (1 - z // middle) if turn == 0 else z // middle
                pair = pl.ds(pl.multiple_of(side * middle * cb, middle * cb), middle * cb)
                es[k][pair, :] = product(turned_3[pair, :], factor[0 : 3 * spots, 0:width], ((1,), (0,)))

            @pl.when(z == 0)
            def _():
                if halved(k):
                    pass_up(k, middle if turn == 0 else 1, middle if turn == 0 else middle - 1, turn)
                elif whole(k):
                    if turn == 0:
                        pass_up(k, 1, last, 0)
                elif turn == 0:
                    for line in range(last, 0, -1):
                        pass_up(k, line, 1, line)

            @pl.when(z == last)
            def _():
                if halved(k):
                    pass_down(k, 0 if turn == 0 else middle, middle if turn == 0 else middle - 1, turn)
                elif whole(k):
                    if turn == 0:
                        pass_down(k, 0, last, 0)
                elif turn == 0:
                    for line in range(last):
                        pass_down(k, line, 1, line)

    def halved(k):
        return k == 0

    def whole(k):
        return 0 < k < turns - SPLIT

    def pass_up(k, line, count, slot):
        here = pl.ds(line * cb, count * cb)
        send(es[k].at[here], ru[k].at[here], ru_s.at[k], ru_r.at[k, slot], up)

    def pass_down(k, line, count, slot):
        here = pl.ds(line * cb, count * cb)
        send(es[k].at[here], rd[k].at[here], rd_s.at[k], rd_r.at[k, slot], down)

    def take_up(k, line, count, slot):
        arrived(ru[k].at[pl.ds(line * cb, count * cb)], ru_r.at[k, slot])

    def take_down(k, line, count, slot):
        arrived(rd[k].at[pl.ds(line * cb, count * cb)], rd_r.at[k, slot])

    def add_up(k, line, count):
        def add(at):
            es[k][at, :] += ru[k][at, :]

        in_blocks(line * cb, count * cb, add)

    def add_down(k, line, count):
        def add(at):
            es[k][at, :] += rd[k][at, :]

        in_blocks(line * cb, count * cb, add)

    def rising(k, at):
        if halved(k) or whole(k):
            start = middle if halved(k) else at
            take_up(k, start, lines - start, 0)
            above = max(at + 1, start)
            add_up(k, above, lines - above)
            pass_up(k, above, lines - above, 0)
        else:
            for line in range(last, at, -1):
                take_up(k, line, 1, line)
                add_up(k, line, 1)
                pass_up(k, line, 1, line)

    def falling(k, at):
        if halved(k) or whole(k):
            end = middle if halved(k) else at + 1
            take_down(k, 0, end, 0)
            below = min(at, end)
            add_down(k, 0, below)
            pass_down(k, 0, below, 0)
        else:
            for line in range(at):
                take_down(k, line, 1, line)
                add_down(k, line, 1)
                pass_down(k, line, 1, line)

    def add_near(k):
        for at in range(1, last):

            @pl.when(z == at)
            def _():
                (rising if low(at) else falling)(k, at)

    def add_far(k):
        for at in range(1, last):

            @pl.when(z == at)
            def _():
                (falling if low(at) else rising)(k, at)

    def finish_expr(k):
        for at in range(lines):

            @pl.when(z == at)
            def _():
                if at > 0:
                    if halved(k) and at < middle:
                        take_up(k, at, 1, 1)
                    elif at == last and (halved(k) or whole(k)):
                        take_up(k, at, 1, 0)
                    elif not halved(k) and not whole(k):
                        take_up(k, at, 1, at)
                if at < last:
                    if halved(k) and at >= middle:
                        take_down(k, at, 1, 1)
                    elif at == 0 and (halved(k) or whole(k)):
                        take_down(k, at, 1, 0)
                    elif not halved(k) and not whole(k):
                        take_down(k, at, 1, at)

        from_low, from_high = z > 0, z < last

        @pl.loop(0, cb // BLOCK)
        def _(step):
            here = pl.ds(pl.multiple_of(step * BLOCK, BLOCK), BLOCK)
            own = pl.ds(pl.multiple_of(z * cb + step * BLOCK, BLOCK), BLOCK)
            total = es[k][own, :]
            total = total + jnp.where(from_low, ru[k][own, :], 0.0)
            ge[here, turn_cols(k)] = total + jnp.where(from_high, rd[k][own, :], 0.0)

    def probs_gradient(k):
        at = three_turn_cols(k)

        @pl.loop(0, PLANE * rows // TALL)
        def _(step):
            tall = pl.ds(pl.multiple_of(step * TALL, TALL), TALL)
            part = product(grad_3[tall, at], expr_3[:, at], ((1,), (1,)))
            if k == 0:
                fs[tall, :] = part
            else:
                fs[tall, :] += part

    def slide_of(p, m):
        return pl.ds(pl.multiple_of(p * rows + m * slide_rows, slide_rows), slide_rows)

    def sum_probs_cores():
        for p in mates + (q,):
            fx[p] = fs[slide_of(p, 1 - core), :]
            send(fx.at[p], fy.at[p], fx_s, fx_r.at[p], sibling)

    def return_probs():
        for p in mates:
            arrived(fy.at[p], fx_r.at[p])
            fz[p] = fs[slide_of(p, core), :] + fy[p]
            send(fz.at[p], fr.at[q], f_s, f_r.at[q], mate(p))
        arrived(fy.at[q], fx_r.at[q])
        fr[q] = fs[slide_of(q, core), :] + fy[q]

    def pass_terms():
        for p in mates:
            arrived(l1.at[p], l1_r.at[p])
        l2[z] = (l1[0] + l1[1]) + (l1[2] + l1[3])
        for o in others:
            send(l2.at[z], l2.at[z], l2_s, l2_r.at[z], (o * PLANE + q, core))

    def part_of(slide, m):
        start = slide * slide_rows + m * (slide_rows // 2)
        return pl.ds(pl.multiple_of(start, slide_rows // 2), slide_rows // 2)

    def finish_logits():
        arrived(inn.at[1 - core], in_r)
        rowv[2] = (inn[0] + inn[1]) + rowv[1] * rowv[0]
        for p in mates:
            arrived(fr.at[p], f_r.at[p])
        for m in range(2):

            @pl.loop(0, slide_rows // STEP_ROWS // 2)
            def _(step):
                row_at = (m * (slide_rows // STEP_ROWS // 2) + step) * STEP_ROWS
                at = pl.ds(pl.multiple_of(row_at, STEP_ROWS), STEP_ROWS)
                whole_at = pl.ds(pl.multiple_of(core * slide_rows + row_at, STEP_ROWS), STEP_ROWS)
                by_mass, total_inner = rowv[1, whole_at, 0:1], rowv[2, whole_at, 0:1]
                for p in range(PLANE):
                    for line in range(lines):
                        here, there = pl.ds(line * cb, cb), (line * PLANE + p) * cb
                        grad = fr[p, at, here] + by_mass * weights[:, there : there + cb]
                        glog[whole_at, pl.ds(there, cb)] = pq[p, whole_at, here] * (grad - total_inner)

            here = part_of(core, m)
            send(glog.at[here], glog.at[here], go_s, go_r.at[m], sibling)

    def forward_left():
        for k in range(chunks):

            @pl.when(z < last)
            def _():
                sent(bb[k].at[block(z)], ou_s.at[k])

            @pl.when(z > 0)
            def _():
                sent(bb[k].at[block(z)], od_s.at[k])

            for at in range(1, last):

                @pl.when(z == at)
                def _():
                    sent(bb[k].at[pl.ds(0, at * cb)], fu_s.at[k])
                    sent(bb[k].at[pl.ds((at + 1) * cb, (last - at) * cb)], fd_s.at[k])

        three = pl.ds(0, len(mates))
        sent(ab.at[three, half(0)], a_s)
        sent(ab.at[three, half(0)], a2_s)
        sent(rs.at[three], r_s)
        sent(t0.at[three], t0_s)
        sent(p0.at[three], p0_s)
        for k in range(chunks):
            sent(cr[k].at[three], c_s.at[k])
        sent(s1.at[three], s1_s)
        sent(s2.at[pl.ds(0, last)], s2_s)
        sent(ss.at[0], ss_s)

    steps = {
        "far": forward_far,
        "near": forward_near,
        "share": share_logits,
        "take": take_probs,
        "whole": gathered,
        "product": forward_product,
        "sum": finish_pred,
        "turn": transpose,
        "plane": sum_plane,
        "line": sum_line,
        "genes": finish_genes,
        "cores": sum_cores,
        "spots": finish_spots,
        "grad": send_grad,
        "terms": send_terms,
        "late": pass_late,
        "backward": backward_product,
        "probs": probs_gradient,
        "exchange": sum_probs_cores,
        "return": return_probs,
        "loss": pass_terms,
        "logits": finish_logits,
        "add_near": add_near,
        "add_far": add_far,
        "expr": finish_expr,
        "left": forward_left,
    }
    for name, *where in STEPS:
        steps[name](*where)

    for o in others:
        arrived(l2.at[o], l2_r.at[o])
    loss = l2[0]
    for line in range(1, lines):
        loss = loss + l2[line]
    loss_ref[...] = loss[0:1, 0:1] - (inn[0, 0:1, 1:2] + inn[1, 0:1, 1:2])
    for m in range(2):
        arrived(glog.at[part_of(1 - core, m)], go_r.at[m])

    for k in range(turns):
        for at in range(lines):

            @pl.when(z == at)
            def _():
                if at < last:
                    sent(es[k].at[pl.ds((at + 1) * cb, (last - at) * cb)], ru_s.at[k])
                if at > 0:
                    sent(es[k].at[pl.ds(0, at * cb)], rd_s.at[k])

    three = pl.ds(0, len(mates))
    for k in range(1, turns):
        sent(ds[k].at[pl.ds(0, len(mates) * rows)], d_s.at[k])
    sent(vr.at[three], vr_s)
    sent(inn.at[0], in_s)
    sent(l1.at[three], l1_s)
    sent(l2.at[pl.ds(0, last)], l2_s)
    sent(fr.at[three], f_s)
    sent(fx, fx_s)
    sent(glog.at[half(0)], go_s)


def lane_groups(value):
    parts = [value[:, at : at + LANES] for at in range(0, value.shape[1], LANES)]
    return functools.reduce(lambda a, b: a + b, parts)


def grouped(refs, sizes):
    at = 0
    for size in sizes:
        yield refs[at : at + size]
        at += size


def deliver(pred_in, loss_in, glog_in, gexp_in, pred_ref, loss_ref, glog_ref, gexp_ref, sems):
    slides, slide_rows = pred_ref.shape[0], pred_ref.shape[1]
    pairs = [(gexp_in, gexp_ref), (loss_in, loss_ref)]
    for m in range(slides):
        part = pl.ds(m * slide_rows, slide_rows)
        pairs += [(glog_in.at[part], glog_ref.at[m]), (pred_in.at[part], pred_ref.at[m])]
    copies = [pltpu.make_async_copy(src, dst, sems.at[at]) for at, (src, dst) in enumerate(pairs)]
    for copy in copies:
        copy.start()
    for copy in copies:
        copy.wait()


def plane_call(logits, expr, spatial, slide_spots, spot_cells, cell_prior, lines):
    slides, slide_rows, cells = logits.shape
    rows = slides * slide_rows
    cb, genes = expr.shape
    quarter = lines * cb
    spots = PLANE * rows
    chunks, turns = len(FORWARD), len(BACKWARD)
    dma = pltpu.SemaphoreType.DMA
    vmem = pltpu.VMEM
    anywhere = pl.BlockSpec(memory_space=pl.ANY)
    in_vmem = pl.BlockSpec(memory_space=pltpu.VMEM)
    scratch = [
        pltpu.SMEM((slides,), jnp.int32),
        vmem((slides, slide_rows), jnp.int32),
        vmem((1, cells), jnp.int32),
        vmem((rows, cells), F32),
        vmem((PLANE, slide_rows, quarter), F32),
        vmem((rows, genes), F32),
        vmem((cb, genes), F32),
        vmem((PLANE, rows, quarter), F32),
        vmem((PLANE, rows, quarter), F32),
        vmem((PLANE, rows, quarter), F32),
        vmem((spots, 3 * quarter), BF16),
        vmem((quarter, 3 * spots), BF16),
        vmem((quarter, 3 * genes), BF16),
        vmem((3, rows, LANES), F32),
        vmem((PLANE, 8, genes), F32),
        vmem((lines, 8, genes), F32),
        vmem((8, genes), F32),
        vmem((2, 8, rows), F32),
        vmem((3, rows, LANES), F32),
        vmem((PLANE, 8, rows), F32),
        vmem((spots, 3 * genes), BF16),
        vmem((3 * max(quarter, spots), max(FORWARD + BACKWARD)), BF16),
        vmem((PLANE, rows, BACKWARD[0]), F32),
        vmem((PLANE, rows, BACKWARD[0]), F32),
        vmem((PLANE, 8, rows), F32),
        vmem((spots, quarter), F32),
        vmem((PLANE, slide_rows, quarter), F32),
        vmem((PLANE, slide_rows, quarter), F32),
        vmem((PLANE, slide_rows, quarter), F32),
        vmem((PLANE, slide_rows, quarter), F32),
        vmem((2, rows, LANES), F32),
        vmem((PLANE, 8, LANES), F32),
        vmem((lines, 8, LANES), F32),
        dma((2 * slides + 4,)),
        dma((chunks,)),
        dma((chunks,)),
        dma((chunks,)),
        dma((chunks,)),
        dma((chunks,)),
        dma((chunks,)),
        dma((chunks,)),
        dma((chunks,)),
        dma,
        dma((PLANE,)),
        dma,
        dma((PLANE,)),
        dma,
        dma((PLANE,)),
        dma((chunks,)),
        dma((chunks, PLANE)),
        dma,
        dma((2, PLANE)),
        dma,
        dma((2, lines)),
        dma,
        dma,
        dma((turns,)),
        dma((turns, PLANE)),
        dma((turns,)),
        dma((turns, lines)),
        dma((turns,)),
        dma((turns, lines)),
        dma,
        dma((PLANE,)),
        dma,
        dma((PLANE,)),
        dma,
        dma((2,)),
        dma,
        dma,
        dma,
        dma((PLANE,)),
        dma,
        dma((lines,)),
        dma,
        dma((PLANE,)),
        dma,
        dma((PLANE,)),
        dma,
        dma((PLANE,)),
    ]
    for shape, widths in (
        ((quarter,), FORWARD),
        ((spots,), FORWARD),
        ((PLANE, rows), FORWARD),
        ((spots,), BACKWARD),
        ((quarter,), BACKWARD),
        ((quarter,), BACKWARD),
        ((quarter,), BACKWARD),
    ):
        scratch += [vmem(shape + (width,), F32) for width in widths]
    in_hbm = functools.partial(pltpu.with_memory_space_constraint, memory_space=pltpu.HBM)
    in_place = functools.partial(pltpu.with_memory_space_constraint, memory_space=pltpu.VMEM)
    results = pl.pallas_call(
        functools.partial(plane_kernel, lines, FORWARD, BACKWARD),
        out_shape=(
            vmem((rows, genes), F32),
            vmem((1, 1), F32),
            vmem((rows, cells), F32),
            vmem((cb, genes), F32),
        ),
        in_specs=[anywhere] * 6,
        out_specs=(in_vmem,) * 4,
        scratch_shapes=scratch,
        compiler_params=pltpu.CompilerParams(
            collective_id=0, has_side_effects=True, vmem_limit_bytes=48 * 1024 * 1024
        ),
    )(*map(in_hbm, (logits, expr, spatial, slide_spots, spot_cells, cell_prior.reshape(1, cells))))
    pred, loss, grad_logits, grad_expr = pl.pallas_call(
        deliver,
        out_shape=(
            jax.ShapeDtypeStruct((slides, slide_rows, genes), F32),
            jax.ShapeDtypeStruct((1, 1), F32),
            jax.ShapeDtypeStruct((slides, slide_rows, cells), F32),
            jax.ShapeDtypeStruct((cb, genes), F32),
        ),
        in_specs=[anywhere] * 4,
        out_specs=(anywhere,) * 4,
        scratch_shapes=[dma((2 * slides + 2,))],
        compiler_params=pltpu.CompilerParams(vmem_limit_bytes=4 * 1024 * 1024),
    )(*map(in_place, results))
    return pred, loss.reshape(()), grad_logits, grad_expr


def general_plan(logits, expr, spatial, slide_spots, spot_cells, cell_prior):
    place = lax.axis_index("spot")
    side = lax.axis_index("gene")
    rows_all = logits.shape[1]
    cell_rows = expr.shape[0]
    weights = cell_prior.astype(jnp.float32) / fixed_point
    gene_share = (place == 0).astype(jnp.float32)
    row_share = (side == 0).astype(jnp.float32)
    own_weights = lax.dynamic_slice_in_dim(weights, place * cell_rows, cell_rows, 0)
    expr_acc = jnp.zeros((cell_rows, expr.shape[1]), jnp.float32)
    loss_local = jnp.zeros((), jnp.float32)
    pred_list = []
    grad_list = []
    for slide in range(logits.shape[0]):
        logit_rows = logits[slide]
        counted = spot_cells[slide].astype(jnp.float32)
        target = spatial[slide]
        positions = place * rows_all + jnp.arange(rows_all, dtype=jnp.int32)
        valid = (positions < slide_spots[slide]).astype(jnp.float32)
        peak = jnp.max(logit_rows, axis=1, keepdims=True)
        raised = jnp.exp(logit_rows - peak)
        probs = raised / jnp.sum(raised, axis=1, keepdims=True)
        mass = jnp.dot(probs, weights, precision=lax.Precision.HIGHEST)
        blocks = lax.all_to_all(probs, "spot", split_axis=1, concat_axis=0, tiled=True)
        pred = lax.psum_scatter(
            jnp.dot(blocks, expr, precision=lax.Precision.HIGHEST),
            "spot",
            scatter_dimension=0,
            tiled=True,
        )
        gene_dot = jnp.sum(valid[:, None] * pred * target, axis=0)
        gene_pred = jnp.sum(valid[:, None] * pred * pred, axis=0)
        gene_true = jnp.sum(valid[:, None] * target * target, axis=0)
        mass_part = jnp.sum(valid * mass)
        kcell = valid * counted
        cell_part = jnp.sum(kcell)
        spot_dot = jnp.sum(pred * target, axis=1)
        spot_pred = jnp.sum(pred * pred, axis=1)
        spot_true = jnp.sum(target * target, axis=1)
        gene_dot, gene_pred, gene_true, mass_total, cell_total = lax.psum(
            (gene_dot, gene_pred, gene_true, mass_part, cell_part), "spot"
        )
        spot_dot, spot_pred, spot_true = lax.psum((spot_dot, spot_pred, spot_true), "gene")
        gene_inv = lax.rsqrt(gene_pred * gene_true + tiny)
        cos_gene = gene_dot * gene_inv
        spot_inv = lax.rsqrt(spot_pred * spot_true + tiny)
        cos_spot = spot_dot * spot_inv
        share = kcell / cell_total
        scale_count = slide_spots[slide].astype(jnp.float32)
        kl_part = jnp.sum(
            share * (jnp.log(counted) - jnp.log(cell_total) - jnp.log(mass) + jnp.log(mass_total))
        )
        loss_local = loss_local - gene_share * jnp.sum(cos_gene)
        loss_local = loss_local + row_share * (scale_count * kl_part - jnp.sum(valid * cos_spot))
        gene_back = cos_gene * gene_true / (gene_pred * gene_true + tiny)
        spot_back = cos_spot * spot_true / (spot_pred * spot_true + tiny)
        dpred = -valid[:, None] * (
            target * (gene_inv[None, :] + spot_inv[:, None])
            - pred * gene_back[None, :]
            - pred * spot_back[:, None]
        )
        dmass = scale_count * valid * (1.0 / mass_total - share / mass)
        pred_list.append(pred)
        grads_full, mass_full = (
            lax.all_gather(dpred, "spot", axis=0, tiled=True),
            lax.all_gather(dmass, "spot", axis=0, tiled=True),
        )
        dprob_cells = jnp.dot(grads_full, expr.T, precision=lax.Precision.HIGHEST)
        dprob_cells = lax.psum(dprob_cells, "gene")
        expr_acc = expr_acc + lax.dot_general(
            blocks, grads_full, (((0,), (0,)), ((), ())), precision=lax.Precision.HIGHEST
        )
        dprob_cells = dprob_cells + mass_full[:, None] * own_weights[None, :]
        dprob_rows = lax.all_to_all(dprob_cells, "spot", split_axis=0, concat_axis=1, tiled=True)
        inner = jnp.sum(probs * dprob_rows, axis=1, keepdims=True)
        dlogit = probs * (dprob_rows - inner)
        grad_list.append(dlogit)
    loss = lax.psum(loss_local, ("spot", "gene"))
    return (jnp.stack(pred_list), loss, jnp.stack(grad_list), expr_acc)


def solution(mesh):
    places = mesh.shape["spot"]

    def on_device(logits, expr, spatial, slide_spots, spot_cells, cell_prior):
        if places == PLANE * PLANE and mesh.shape["gene"] == 2 and expr.shape[1] == sum(FORWARD):
            return plane_call(
                logits, expr, spatial, slide_spots, spot_cells, cell_prior, places // PLANE
            )
        return general_plan(logits, expr, spatial, slide_spots, spot_cells, cell_prior)

    in_specs = (
        P(None, "spot", None),
        P("spot", "gene"),
        P(None, "spot", "gene"),
        P(),
        P(None, "spot"),
        P(),
    )
    out_specs = (P(None, "spot", "gene"), P(), P(None, "spot", None), P("spot", "gene"))
    return jax.shard_map(
        on_device, mesh=mesh, in_specs=in_specs, out_specs=out_specs, check_vma=False
    )
```

```python
import functools

import jax
import jax.numpy as jnp
from jax import lax
from jax.experimental import pallas as pl
from jax.experimental.pallas import tpu as pltpu
from jax.sharding import PartitionSpec as P

tiny = 1e-06
fixed_point = 16384.0
F32 = jnp.float32
BF16 = jnp.bfloat16
MESH = pl.DeviceIdType.MESH

PLANE = 4
LANES = 128
STEP_ROWS = 16
BLOCK = 32
TALL = 256
FORWARD = (128, 256, 256, 128, 128, 128)
BACKWARD = (128, 128, 256, 256, 256)
SPLIT = 2
LEAD = 2
NEAR_LEAD = 3
EARLY = 3
STEPS = (
    ("far", 0),
    ("far", 1),
    ("near", 0),
    ("share",),
    ("far", 2),
    ("far", 3),
    ("take",),
    ("whole", 0),
    ("near", 1),
    ("product", 0),
    ("sum", 0),
    ("whole", 1),
    ("near", 2),
    ("product", 1),
    ("whole", 2),
    ("product", 2),
    ("whole", 3),
    ("near", 3),
    ("product", 3),
    ("far", 4),
    ("whole", 4),
    ("near", 4),
    ("product", 4),
    ("sum", 1),
    ("turn", 0),
    ("far", 5),
    ("whole", 5),
    ("near", 5),
    ("product", 5),
    ("sum", 2),
    ("plane", 0),
    ("turn", 1),
    ("sum", 3),
    ("line", 0),
    ("sum", 4),
    ("sum", 5),
    ("plane", 1),
    ("cores",),
    ("genes", 0),
    ("spots",),
    ("grad", 0),
    ("grad", 1),
    ("grad", 2),
    ("line", 1),
    ("backward", 0),
    ("backward", 1),
    ("add_near", 0),
    ("genes", 1),
    ("grad", 3),
    ("backward", 2),
    ("probs", 0),
    ("add_far", 0),
    ("probs", 1),
    ("expr", 0),
    ("grad", 4),
    ("add_near", 1),
    ("probs", 2),
    ("terms",),
    ("backward", 3),
    ("probs", 3),
    ("add_near", 2),
    ("backward", 4),
    ("add_far", 1),
    ("probs", 4),
    ("exchange",),
    ("add_near", 3),
    ("add_far", 2),
    ("left",),
    ("return",),
    ("loss",),
    ("add_far", 3),
    ("expr", 1),
    ("add_near", 4),
    ("logits",),
    ("add_far", 4),
    ("expr", 2),
    ("expr", 3),
    ("expr", 4),
)


def halves(value):
    high = value.astype(BF16)
    return high, (value - high.astype(F32)).astype(BF16)


def threefold(value):
    high, low = halves(value)
    return jnp.concatenate([high, high, low], axis=1)


def product(a, b, contract):
    return lax.dot_general(a, b, (contract, ((), ())), preferred_element_type=F32)


def plane_kernel(lines, forward_widths, backward_widths, *refs):
    chunks, turns = len(forward_widths), len(backward_widths)
    (
        (logits_ref, expr_ref, spatial_ref, count_in, cells_in, prior_in),
        (pr, loss_ref, glog, ge),
        (count_ref, cells_ref, prior_ref, lg, lq, tg, ex, pq, ab, af, probs_3, turned_3, expr_3, sacc, s1, s2, gv, ss, rowv, rs),
        (grad_3, factor, t0, p0, vr, fs, fx, fy, fz, fr, inn, l1, l2),
        (loc, ou_s, ou_r, od_s, od_r, fu_s, fu_r, fd_s, fd_r, a_s, a_r, a2_s, a2_r, r_s, r_r),
        (c_s, c_r, s1_s, s1_r, s2_s, s2_r, ss_s, ss_r, d_s, d_r, ru_s, ru_r, rd_s, rd_r),
        (f_s, f_r, fx_s, fx_r, go_s, go_r, in_s, in_r, l1_s, l1_r, l2_s, l2_r, t0_s, t0_r, p0_s, p0_r, vr_s, vr_r),
        bb,
        cs,
        cr,
        ds,
        es,
        ru,
        rd,
    ) = grouped(refs, (6, 4, 20, 13, 15, 14, 18, chunks, chunks, chunks, turns, turns, turns, turns))
    place = lax.axis_index("spot")
    core = lax.axis_index("gene")
    z = place // PLANE
    q = place % PLANE
    col, row = q % 2, q // 2
    mates = ((1 - row) * 2 + 1 - col, row * 2 + 1 - col, (1 - row) * 2 + col)
    others = tuple((z + step) % lines for step in range(1, lines))
    up, down = (place + PLANE, core), (place - PLANE, core)
    sibling = (place, 1 - core)
    slides, slide_rows = logits_ref.shape[0], logits_ref.shape[1]
    rows = slides * slide_rows
    cb = expr_ref.shape[0]
    genes = expr_ref.shape[1]
    last = lines - 1

    def mate(p):
        return (z * PLANE + p, core)

    def send(src, dst, send_sem, recv_sem, device):
        copy = pltpu.make_async_remote_copy(
            src_ref=src, dst_ref=dst, send_sem=send_sem, recv_sem=recv_sem, device_id=device, device_id_type=MESH
        )
        copy.start()

    def arrived(dst, recv_sem):
        pltpu.make_async_copy(dst, dst, recv_sem).wait()

    sent = arrived

    def cols(k):
        return pl.ds(sum(forward_widths[:k]), forward_widths[k])

    def turn_cols(k):
        return pl.ds(sum(backward_widths[:k]), backward_widths[k])

    def block(index):
        return pl.ds(pl.multiple_of(index * cb, cb), cb)

    def share(index):
        return pl.ds(pl.multiple_of(index * rows, rows), rows)

    def half(index):
        return pl.ds(pl.multiple_of(index * slide_rows, slide_rows), slide_rows)

    small = ((prior_in, prior_ref), (count_in, count_ref), (cells_in, cells_ref))
    pltpu.make_async_copy(expr_ref, ex, loc.at[2 * slides]).start()
    for m in range(slides):
        pltpu.make_async_copy(logits_ref.at[m], lg.at[half(m)], loc.at[m]).start()
    for at, (src, dst) in enumerate(small):
        pltpu.make_async_copy(src, dst, loc.at[2 * slides + 1 + at]).start()
    for m in range(slides):
        pltpu.make_async_copy(spatial_ref.at[m], tg.at[half(m)], loc.at[slides + m]).start()

    barrier = pltpu.get_barrier_semaphore()
    for p in mates:
        pl.semaphore_signal(barrier, inc=1, device_id=mate(p), device_id_type=MESH)
    for o in others:
        pl.semaphore_signal(barrier, inc=1, device_id=(o * PLANE + q, core), device_id_type=MESH)
    pl.semaphore_signal(barrier, inc=1, device_id=sibling, device_id_type=MESH)
    pltpu.make_async_copy(expr_ref, ex, loc.at[2 * slides]).wait()
    for k in range(chunks):
        bb[k][block(z), :] = ex[:, cols(k)]
    for m in range(slides):
        pltpu.make_async_copy(logits_ref.at[m], lg.at[half(m)], loc.at[m]).wait()
    for p in range(PLANE):
        for line in range(lines):
            lq[p, :, pl.ds(line * cb, cb)] = lg[half(core), pl.ds((line * PLANE + p) * cb, cb)]
    pl.semaphore_wait(barrier, len(mates) + len(others) + 1)

    def own_up(k):
        here = bb[k].at[block(z)]
        send(here, here, ou_s.at[k], ou_r.at[k], up)

    def own_down(k):
        here = bb[k].at[block(z)]
        send(here, here, od_s.at[k], od_r.at[k], down)

    def low(at):
        return 2 * at < lines

    for at in range(lines):

        @pl.when(z == at)
        def _():
            for k in range(chunks):
                if at < last and (at == 0 or k < (LEAD if low(at) else NEAR_LEAD)):
                    own_up(k)
                if at > 0 and (at == last or k < (NEAR_LEAD if low(at) else LEAD)):
                    own_down(k)

    for p in mates:
        send(lq.at[p], ab.at[q, half(core)], a_s, a_r.at[q], mate(p))

    def from_below(k, at):
        arrived(bb[k].at[pl.ds((at - 1) * cb, cb)], ou_r.at[k])
        if at > 1:
            arrived(bb[k].at[pl.ds(0, (at - 1) * cb)], fu_r.at[k])

    def from_above(k, at):
        arrived(bb[k].at[pl.ds((at + 1) * cb, cb)], od_r.at[k])
        if at < last - 1:
            arrived(bb[k].at[pl.ds((at + 2) * cb, (last - 1 - at) * cb)], fd_r.at[k])

    def upward(k, at):
        from_below(k, at)
        here = bb[k].at[pl.ds(0, at * cb)]
        send(here, here, fu_s.at[k], fu_r.at[k], up)

    def downward(k, at):
        from_above(k, at)
        here = bb[k].at[pl.ds((at + 1) * cb, (last - at) * cb)]
        send(here, here, fd_s.at[k], fd_r.at[k], down)

    def forward_far(k):
        for at in range(1, last):

            @pl.when(z == at)
            def _():
                (upward if low(at) else downward)(k, at)
                if k + LEAD < chunks:
                    (own_up if low(at) else own_down)(k + LEAD)

    def forward_near(k):
        for at in range(1, last):

            @pl.when(z == at)
            def _():
                (downward if low(at) else upward)(k, at)
                if k + NEAR_LEAD < chunks:
                    (own_down if low(at) else own_up)(k + NEAR_LEAD)

    def gathered(k):
        @pl.when(z == 0)
        def _():
            from_above(k, 0)

        @pl.when(z == last)
        def _():
            from_below(k, last)

    for at, (src, dst) in enumerate(small):
        pltpu.make_async_copy(src, dst, loc.at[2 * slides + 1 + at]).wait()
    weights = prior_ref[...].astype(F32) / fixed_point

    @pl.loop(0, rows // STEP_ROWS)
    def _(step):
        at = pl.ds(pl.multiple_of(step * STEP_ROWS, STEP_ROWS), STEP_ROWS)
        value = lg[at, :]
        peak = jnp.max(value, axis=1, keepdims=True)
        raised = jnp.exp(value - peak)
        scale = 1.0 / jnp.sum(raised, axis=1, keepdims=True)
        probs = raised * scale
        mass_rows = jnp.sum(probs * weights, axis=1, keepdims=True)
        rowv[0, at, :] = jnp.broadcast_to(mass_rows, (STEP_ROWS, LANES))
        rowv[1, at, :] = jnp.broadcast_to(peak, (STEP_ROWS, LANES))
        rowv[2, at, :] = jnp.broadcast_to(scale, (STEP_ROWS, LANES))
        for p in range(PLANE):
            for line in range(lines):
                at_cells = (line * PLANE + p) * cb
                pq[p, at, pl.ds(line * cb, cb)] = probs[:, at_cells : at_cells + cb]

    wide = lax.broadcasted_iota(jnp.int32, (rows, LANES), 1)
    rs[q] = jnp.where(wide == 0, rowv[1], rowv[2]).T[0:8]
    for p in mates:
        send(rs.at[q], rs.at[q], r_s, r_r.at[q], mate(p))

    rid = lax.broadcasted_iota(jnp.int32, (rows, 1), 0)
    first = rid < slide_rows
    position = place * slide_rows + jnp.where(first, rid, rid - slide_rows)
    count = jnp.where(first, count_ref[0], count_ref[1])
    valid = (position < count).astype(F32)
    scale_count = count.astype(F32)
    square = (slide_rows, slide_rows)
    eye = lax.broadcasted_iota(jnp.int32, square, 0) == lax.broadcasted_iota(jnp.int32, square, 1)
    counted = jnp.concatenate(
        [
            jnp.sum(jnp.where(eye, cells_ref[m : m + 1, :].astype(F32), 0.0), axis=1, keepdims=True)
            for m in range(slides)
        ],
        axis=0,
    )
    mass = rowv[0, :, 0:1]
    kcell = valid * counted

    def by_slide(value):
        return [jnp.sum(value[m * slide_rows : (m + 1) * slide_rows], axis=0, keepdims=True) for m in range(slides)]

    mass_parts = by_slide(valid * mass)
    cell_parts = by_slide(kcell)
    lane = lax.broadcasted_iota(jnp.int32, (1, LANES), 1)
    scalars = jnp.zeros((1, LANES), F32)
    for at, value in enumerate(mass_parts + cell_parts):
        scalars = jnp.where(lane == at, value, scalars)
    for m in range(slides):
        pltpu.make_async_copy(spatial_ref.at[m], tg.at[half(m)], loc.at[slides + m]).wait()

    head = backward_widths[0]
    t0[q] = tg[:, 0:head]
    for p in mates:
        send(t0.at[q], t0.at[q], t0_s, t0_r.at[q], mate(p))
    sacc[...] = jnp.zeros_like(sacc)
    s1[q, 3 * slides :, :] = jnp.zeros((8 - 3 * slides, genes), F32)
    s1[q, 3 * slides : 3 * slides + 1, 0:LANES] = scalars

    def share_logits():
        for p in (mates[1], mates[2], mates[0]):
            here = ab.at[p, half(core)]
            arrived(here, a_r.at[p])
            send(here, here, a2_s, a2_r.at[p], sibling)

    def lay_probs(p, at, value):
        af[p, at, :] = value
        there = pl.ds(pl.multiple_of(p * rows + at.start, BLOCK), BLOCK)
        probs_3[there, :] = threefold(value)

    def take_probs():
        in_blocks(0, rows, lambda at: lay_probs(q, at, pq[q, at, :]))
        for p in (mates[1], mates[2], mates[0]):
            arrived(rs.at[p], r_r.at[p])
            arrived(ab.at[p, half(1 - core)], a2_r.at[p])
            rowv[1] = jnp.concatenate([rs[p].T, jnp.zeros((rows, LANES - 8), F32)], axis=1)

            def take(at):
                probs = jnp.exp(ab[p, at, :] - rowv[1, at, 0:1]) * rowv[1, at, 1:2]
                lay_probs(p, at, probs)

            in_blocks(0, rows, take)

    def transpose(part):
        @pl.loop(0, PLANE // 2)
        def _(step):
            p = part * (PLANE // 2) + step
            high, low_part = halves(af[p].T)
            for third, value in enumerate((high, high, low_part)):
                turned_3[:, pl.ds(pl.multiple_of(third * PLANE * rows + p * rows, rows), rows)] = value

    def in_blocks(start, count, body):
        @pl.loop(0, count // BLOCK)
        def _(step):
            body(pl.ds(pl.multiple_of(start + step * BLOCK, BLOCK), BLOCK))

    quarter = lines * cb

    def lay_factor(at, length, width, value):
        high, low_part = halves(value)
        for third, part in enumerate((high, low_part, high)):
            here = pl.ds(pl.multiple_of(third * length + at.start, BLOCK), BLOCK)
            factor[here, 0:width] = part

    def keep_expr(k, at, value):
        start = sum(forward_widths[:k])
        for turn in range(turns):
            origin, width = sum(backward_widths[:turn]), backward_widths[turn]
            lo, hi = max(start, origin), min(start + forward_widths[k], origin + width)
            if lo < hi:
                high, low_part = halves(value[:, lo - start : hi - start])
                for third, part in enumerate((high, low_part, high)):
                    expr_3[at, pl.ds(3 * origin + third * width + lo - origin, hi - lo)] = part

    def three_turn_cols(k):
        return pl.ds(3 * sum(backward_widths[:k]), 3 * backward_widths[k])

    def forward_product(k):
        width = forward_widths[k]

        def lay(at):
            value = bb[k][at, :]
            lay_factor(at, quarter, width, value)
            keep_expr(k, at, value)

        in_blocks(0, quarter, lay)
        if k < chunks - 1:

            @pl.loop(0, PLANE * rows // TALL)
            def _(step):
                tall = pl.ds(pl.multiple_of(step * TALL, TALL), TALL)
                cs[k][tall, :] = product(probs_3[tall, :], factor[0 : 3 * quarter, 0:width], ((1,), (0,)))

            for p in mates:
                pass_pred(k, p)
        else:
            for side, served in ((1 - row, (mates[0], mates[2])), (row, (mates[1],))):
                pair = pl.ds(pl.multiple_of(2 * side * rows, 2 * rows), 2 * rows)
                cs[k][pair, :] = product(probs_3[pair, :], factor[0 : 3 * quarter, 0:width], ((1,), (0,)))
                for p in served:
                    pass_pred(k, p)

    def pass_pred(k, p):
        send(cs[k].at[share(p)], cr[k].at[q], c_s.at[k], c_r.at[k, q], mate(p))

    def finish_pred(k):
        total = cs[k][share(q), :]
        for p in mates:
            arrived(cr[k].at[p], c_r.at[k, p])
            total = total + cr[k][p]
        pr[:, cols(k)] = total
        if k == 0:
            p0[q] = total[:, 0:head]
            for p in mates:
                send(p0.at[q], p0.at[q], p0_s, p0_r.at[q], mate(p))
        truth = tg[:, cols(k)]
        for at, value in enumerate((total * truth, total * total, truth * truth)):
            sacc[at] += lane_groups(value)
        kept = valid * total
        stats = by_slide(kept * truth) + by_slide(kept * total) + by_slide(valid * truth * truth)
        s1[q, 0 : 3 * slides, cols(k)] = jnp.concatenate(stats, axis=0)

    early = sum(forward_widths[:EARLY])
    parts = (pl.ds(0, early), pl.ds(early, genes - early))

    def sum_plane(at):
        for p in mates:
            send(s1.at[q, :, parts[at]], s1.at[q, :, parts[at]], s1_s, s1_r.at[at, q], mate(p))

    def sum_line(at):
        for p in mates:
            arrived(s1.at[p, :, parts[at]], s1_r.at[at, p])
        s2[z, :, parts[at]] = (s1[0, :, parts[at]] + s1[1, :, parts[at]]) + (s1[2, :, parts[at]] + s1[3, :, parts[at]])
        for o in others:
            send(s2.at[z, :, parts[at]], s2.at[z, :, parts[at]], s2_s, s2_r.at[at, z], (o * PLANE + q, core))

    kept = {}

    def finish_genes(at):
        for o in others:
            arrived(s2.at[o, :, parts[at]], s2_r.at[at, o])
        total = s2[0, :, parts[at]]
        for line in range(1, lines):
            total = total + s2[line, :, parts[at]]
        gene_dot, gene_pred, gene_true = total[0:2], total[2:4], total[4:6]
        gene_inv = lax.rsqrt(gene_pred * gene_true + tiny)
        cos_gene = gene_dot * gene_inv
        gv[0:2, parts[at]] = gene_inv
        gv[2:4, parts[at]] = cos_gene * gene_true / (gene_pred * gene_true + tiny)
        kept["genes", at] = jnp.sum(jnp.sum(cos_gene, axis=1, keepdims=True), axis=0, keepdims=True)
        if at == 0:
            kept["mass"] = jnp.where(first, total[6:7, 0:1], total[6:7, 1:2])
            kept["cells"] = jnp.where(first, total[6:7, 2:3], total[6:7, 3:4])

    def sum_cores():
        sums = [jnp.sum(sacc[at], axis=1, keepdims=True) for at in range(3)]
        ss[core] = jnp.where(wide == 0, sums[0], jnp.where(wide == 1, sums[1], sums[2])).T[0:8]
        send(ss.at[core], ss.at[core], ss_s, ss_r, sibling)

    def finish_spots():
        lane_id = lax.broadcasted_iota(jnp.int32, (1, rows), 1)
        first_lane = lane_id < slide_rows
        lane_position = place * slide_rows + jnp.where(first_lane, lane_id, lane_id - slide_rows)
        lane_valid = (lane_position < jnp.where(first_lane, count_ref[0], count_ref[1])).astype(F32)
        arrived(ss.at[1 - core], ss_r)
        spot = ss[0] + ss[1]
        spot_dot, spot_pred, spot_true = spot[0:1], spot[1:2], spot[2:3]
        spot_inv = lax.rsqrt(spot_pred * spot_true + tiny)
        cos_spot = spot_dot * spot_inv
        spot_back = cos_spot * spot_true / (spot_pred * spot_true + tiny)
        kept["cos"] = jnp.sum(lane_valid * cos_spot, axis=1, keepdims=True)
        vectors = [lane_valid * spot_inv, lane_valid * spot_back, lane_valid, jnp.zeros((5, rows), F32)]
        vr[q] = jnp.concatenate(vectors, axis=0)
        sacc[0] = jnp.zeros_like(sacc[0])

    def gradient(truth, guess, by_row, k):
        pieces = []
        for m in range(slides):
            lo, hi = m * slide_rows, (m + 1) * slide_rows
            inverse, back = gv[m : m + 1, turn_cols(k)], gv[2 + m : 3 + m, turn_cols(k)]
            spot_inv, spot_back, spot_valid = by_row[lo:hi, 0:1], by_row[lo:hi, 1:2], by_row[lo:hi, 2:3]
            pieces.append(
                guess[lo:hi] * (spot_valid * back + spot_back) - truth[lo:hi] * (spot_valid * inverse + spot_inv)
            )
        return jnp.concatenate(pieces, axis=0)

    def head_gradient():
        for p in mates:
            arrived(t0.at[p], t0_r.at[p])
            arrived(p0.at[p], p0_r.at[p])
            arrived(vr.at[p], vr_r.at[p])
        for p in range(PLANE):
            ds[0][share(p), :] = gradient(t0[p], p0[p], vr[p].T, 0)
        sacc[0] += lane_groups(ds[0][share(q), :] * p0[q])

    def send_grad(k):
        if k == 0:
            for p in mates:
                send(vr.at[q], vr.at[q], vr_s, vr_r.at[q], mate(p))
            kept["by_row"] = vr[q].T
            return
        grad = gradient(tg[:, turn_cols(k)], pr[:, turn_cols(k)], kept["by_row"], k)
        here = ds[k].at[share(q)]
        here[...] = grad
        for p in mates:
            send(here, here, d_s.at[k], d_r.at[k, q], mate(p))
        sacc[0] += lane_groups(grad * pr[:, turn_cols(k)])

    def send_terms():
        mass_total, cell_total = kept["mass"], kept["cells"]
        portion = kcell / cell_total
        kl_rows = portion * (jnp.log(counted) - jnp.log(cell_total) - jnp.log(mass) + jnp.log(mass_total))
        dmass = scale_count * valid * (1.0 / mass_total - portion / mass)
        terms = jnp.sum(scale_count * kl_rows, axis=0, keepdims=True) - kept["cos"]
        l1[q] = jnp.broadcast_to(terms, (8, LANES))
        for p in mates:
            send(l1.at[q], l1.at[q], l1_s, l1_r.at[q], mate(p))
        inner = jnp.sum(sacc[0], axis=1, keepdims=True)
        inn[core] = jnp.where(wide == 0, inner, kept["genes", 0] + kept["genes", 1])
        send(inn.at[core], inn.at[core], in_s, in_r, sibling)
        rowv[1] = jnp.broadcast_to(dmass, (rows, LANES))

    middle = lines // 2

    def backward_product(k):
        if k == 0:
            head_gradient()
        else:
            for p in mates:
                arrived(ds[k].at[share(p)], d_r.at[k, p])
        width, spots = backward_widths[k], PLANE * rows

        def lay(at):
            value = ds[k][at, :]
            lay_factor(at, spots, width, value)
            grad_3[at, three_turn_cols(k)] = threefold(value)

        in_blocks(0, spots, lay)
        if not halved(k):

            @pl.loop(0, quarter // TALL)
            def _(step):
                tall = pl.ds(pl.multiple_of(step * TALL, TALL), TALL)
                es[k][tall, :] = product(turned_3[tall, :], factor[0 : 3 * spots, 0:width], ((1,), (0,)))

        for turn in range(2):
            if halved(k):
                side = (1 - z // middle) if turn == 0 else z // middle
                pair = pl.ds(pl.multiple_of(side * middle * cb, middle * cb), middle * cb)
                es[k][pair, :] = product(turned_3[pair, :], factor[0 : 3 * spots, 0:width], ((1,), (0,)))

            @pl.when(z == 0)
            def _():
                if halved(k):
                    pass_up(k, middle if turn == 0 else 1, middle if turn == 0 else middle - 1, turn)
                elif whole(k):
                    if turn == 0:
                        pass_up(k, 1, last, 0)
                elif turn == 0:
                    for line in range(last, 0, -1):
                        pass_up(k, line, 1, line)

            @pl.when(z == last)
            def _():
                if halved(k):
                    pass_down(k, 0 if turn == 0 else middle, middle if turn == 0 else middle - 1, turn)
                elif whole(k):
                    if turn == 0:
                        pass_down(k, 0, last, 0)
                elif turn == 0:
                    for line in range(last):
                        pass_down(k, line, 1, line)

    def halved(k):
        return k == 0

    def whole(k):
        return 0 < k < turns - SPLIT

    def pass_up(k, line, count, slot):
        here = pl.ds(line * cb, count * cb)
        send(es[k].at[here], ru[k].at[here], ru_s.at[k], ru_r.at[k, slot], up)

    def pass_down(k, line, count, slot):
        here = pl.ds(line * cb, count * cb)
        send(es[k].at[here], rd[k].at[here], rd_s.at[k], rd_r.at[k, slot], down)

    def take_up(k, line, count, slot):
        arrived(ru[k].at[pl.ds(line * cb, count * cb)], ru_r.at[k, slot])

    def take_down(k, line, count, slot):
        arrived(rd[k].at[pl.ds(line * cb, count * cb)], rd_r.at[k, slot])

    def add_up(k, line, count):
        def add(at):
            es[k][at, :] += ru[k][at, :]

        in_blocks(line * cb, count * cb, add)

    def add_down(k, line, count):
        def add(at):
            es[k][at, :] += rd[k][at, :]

        in_blocks(line * cb, count * cb, add)

    def rising(k, at):
        if halved(k) or whole(k):
            start = middle if halved(k) else at
            take_up(k, start, lines - start, 0)
            above = max(at + 1, start)
            add_up(k, above, lines - above)
            pass_up(k, above, lines - above, 0)
        else:
            for line in range(last, at, -1):
                take_up(k, line, 1, line)
                add_up(k, line, 1)
                pass_up(k, line, 1, line)

    def falling(k, at):
        if halved(k) or whole(k):
            end = middle if halved(k) else at + 1
            take_down(k, 0, end, 0)
            below = min(at, end)
            add_down(k, 0, below)
            pass_down(k, 0, below, 0)
        else:
            for line in range(at):
                take_down(k, line, 1, line)
                add_down(k, line, 1)
                pass_down(k, line, 1, line)

    def add_near(k):
        for at in range(1, last):

            @pl.when(z == at)
            def _():
                (rising if low(at) else falling)(k, at)

    def add_far(k):
        for at in range(1, last):

            @pl.when(z == at)
            def _():
                (falling if low(at) else rising)(k, at)

    def finish_expr(k):
        for at in range(lines):

            @pl.when(z == at)
            def _():
                if at > 0:
                    if halved(k) and at < middle:
                        take_up(k, at, 1, 1)
                    elif at == last and (halved(k) or whole(k)):
                        take_up(k, at, 1, 0)
                    elif not halved(k) and not whole(k):
                        take_up(k, at, 1, at)
                if at < last:
                    if halved(k) and at >= middle:
                        take_down(k, at, 1, 1)
                    elif at == 0 and (halved(k) or whole(k)):
                        take_down(k, at, 1, 0)
                    elif not halved(k) and not whole(k):
                        take_down(k, at, 1, at)

        from_low, from_high = z > 0, z < last

        @pl.loop(0, cb // BLOCK)
        def _(step):
            here = pl.ds(pl.multiple_of(step * BLOCK, BLOCK), BLOCK)
            own = pl.ds(pl.multiple_of(z * cb + step * BLOCK, BLOCK), BLOCK)
            total = es[k][own, :]
            total = total + jnp.where(from_low, ru[k][own, :], 0.0)
            ge[here, turn_cols(k)] = total + jnp.where(from_high, rd[k][own, :], 0.0)

    def probs_gradient(k):
        at = three_turn_cols(k)

        @pl.loop(0, PLANE * rows // TALL)
        def _(step):
            tall = pl.ds(pl.multiple_of(step * TALL, TALL), TALL)
            part = product(grad_3[tall, at], expr_3[:, at], ((1,), (1,)))
            if k == 0:
                fs[tall, :] = part
            else:
                fs[tall, :] += part

    def slide_of(p, m):
        return pl.ds(pl.multiple_of(p * rows + m * slide_rows, slide_rows), slide_rows)

    def sum_probs_cores():
        for p in mates + (q,):
            fx[p] = fs[slide_of(p, 1 - core), :]
            send(fx.at[p], fy.at[p], fx_s, fx_r.at[p], sibling)

    def return_probs():
        for p in mates:
            arrived(fy.at[p], fx_r.at[p])
            fz[p] = fs[slide_of(p, core), :] + fy[p]
            send(fz.at[p], fr.at[q], f_s, f_r.at[q], mate(p))
        arrived(fy.at[q], fx_r.at[q])
        fr[q] = fs[slide_of(q, core), :] + fy[q]

    def pass_terms():
        for p in mates:
            arrived(l1.at[p], l1_r.at[p])
        l2[z] = (l1[0] + l1[1]) + (l1[2] + l1[3])
        for o in others:
            send(l2.at[z], l2.at[z], l2_s, l2_r.at[z], (o * PLANE + q, core))

    def part_of(slide, m):
        start = slide * slide_rows + m * (slide_rows // 2)
        return pl.ds(pl.multiple_of(start, slide_rows // 2), slide_rows // 2)

    def finish_logits():
        arrived(inn.at[1 - core], in_r)
        rowv[2] = (inn[0] + inn[1]) + rowv[1] * rowv[0]
        for p in mates:
            arrived(fr.at[p], f_r.at[p])
        for m in range(2):

            @pl.loop(0, slide_rows // STEP_ROWS // 2)
            def _(step):
                row_at = (m * (slide_rows // STEP_ROWS // 2) + step) * STEP_ROWS
                at = pl.ds(pl.multiple_of(row_at, STEP_ROWS), STEP_ROWS)
                whole_at = pl.ds(pl.multiple_of(core * slide_rows + row_at, STEP_ROWS), STEP_ROWS)
                by_mass, total_inner = rowv[1, whole_at, 0:1], rowv[2, whole_at, 0:1]
                for p in range(PLANE):
                    for line in range(lines):
                        here, there = pl.ds(line * cb, cb), (line * PLANE + p) * cb
                        grad = fr[p, at, here] + by_mass * weights[:, there : there + cb]
                        glog[whole_at, pl.ds(there, cb)] = pq[p, whole_at, here] * (grad - total_inner)

            here = part_of(core, m)
            send(glog.at[here], glog.at[here], go_s, go_r.at[m], sibling)

    def forward_left():
        for k in range(chunks):

            @pl.when(z < last)
            def _():
                sent(bb[k].at[block(z)], ou_s.at[k])

            @pl.when(z > 0)
            def _():
                sent(bb[k].at[block(z)], od_s.at[k])

            for at in range(1, last):

                @pl.when(z == at)
                def _():
                    sent(bb[k].at[pl.ds(0, at * cb)], fu_s.at[k])
                    sent(bb[k].at[pl.ds((at + 1) * cb, (last - at) * cb)], fd_s.at[k])

        three = pl.ds(0, len(mates))
        sent(ab.at[three, half(0)], a_s)
        sent(ab.at[three, half(0)], a2_s)
        sent(rs.at[three], r_s)
        sent(t0.at[three], t0_s)
        sent(p0.at[three], p0_s)
        for k in range(chunks):
            sent(cr[k].at[three], c_s.at[k])
        sent(s1.at[three], s1_s)
        sent(s2.at[pl.ds(0, last)], s2_s)
        sent(ss.at[0], ss_s)

    steps = {
        "far": forward_far,
        "near": forward_near,
        "share": share_logits,
        "take": take_probs,
        "whole": gathered,
        "product": forward_product,
        "sum": finish_pred,
        "turn": transpose,
        "plane": sum_plane,
        "line": sum_line,
        "genes": finish_genes,
        "cores": sum_cores,
        "spots": finish_spots,
        "grad": send_grad,
        "terms": send_terms,
        "backward": backward_product,
        "probs": probs_gradient,
        "exchange": sum_probs_cores,
        "return": return_probs,
        "loss": pass_terms,
        "logits": finish_logits,
        "add_near": add_near,
        "add_far": add_far,
        "expr": finish_expr,
        "left": forward_left,
    }
    for name, *where in STEPS:
        steps[name](*where)

    for o in others:
        arrived(l2.at[o], l2_r.at[o])
    loss = l2[0]
    for line in range(1, lines):
        loss = loss + l2[line]
    loss_ref[...] = loss[0:1, 0:1] - (inn[0, 0:1, 1:2] + inn[1, 0:1, 1:2])
    for m in range(2):
        arrived(glog.at[part_of(1 - core, m)], go_r.at[m])

    for k in range(turns):
        for at in range(lines):

            @pl.when(z == at)
            def _():
                if at < last:
                    sent(es[k].at[pl.ds((at + 1) * cb, (last - at) * cb)], ru_s.at[k])
                if at > 0:
                    sent(es[k].at[pl.ds(0, at * cb)], rd_s.at[k])

    three = pl.ds(0, len(mates))
    for k in range(1, turns):
        sent(ds[k].at[pl.ds(0, len(mates) * rows)], d_s.at[k])
    sent(vr.at[three], vr_s)
    sent(inn.at[0], in_s)
    sent(l1.at[three], l1_s)
    sent(l2.at[pl.ds(0, last)], l2_s)
    sent(fr.at[three], f_s)
    sent(fx, fx_s)
    sent(glog.at[half(0)], go_s)


def lane_groups(value):
    parts = [value[:, at : at + LANES] for at in range(0, value.shape[1], LANES)]
    return functools.reduce(lambda a, b: a + b, parts)


def grouped(refs, sizes):
    at = 0
    for size in sizes:
        yield refs[at : at + size]
        at += size


def deliver(pred_in, loss_in, glog_in, gexp_in, pred_ref, loss_ref, glog_ref, gexp_ref, sems):
    slides, slide_rows = pred_ref.shape[0], pred_ref.shape[1]
    pairs = [(gexp_in, gexp_ref), (loss_in, loss_ref)]
    for m in range(slides):
        part = pl.ds(m * slide_rows, slide_rows)
        pairs += [(glog_in.at[part], glog_ref.at[m]), (pred_in.at[part], pred_ref.at[m])]
    copies = [pltpu.make_async_copy(src, dst, sems.at[at]) for at, (src, dst) in enumerate(pairs)]
    for copy in copies:
        copy.start()
    for copy in copies:
        copy.wait()


def plane_call(logits, expr, spatial, slide_spots, spot_cells, cell_prior, lines):
    slides, slide_rows, cells = logits.shape
    rows = slides * slide_rows
    cb, genes = expr.shape
    quarter = lines * cb
    spots = PLANE * rows
    chunks, turns = len(FORWARD), len(BACKWARD)
    dma = pltpu.SemaphoreType.DMA
    vmem = pltpu.VMEM
    anywhere = pl.BlockSpec(memory_space=pl.ANY)
    in_vmem = pl.BlockSpec(memory_space=pltpu.VMEM)
    scratch = [
        pltpu.SMEM((slides,), jnp.int32),
        vmem((slides, slide_rows), jnp.int32),
        vmem((1, cells), jnp.int32),
        vmem((rows, cells), F32),
        vmem((PLANE, slide_rows, quarter), F32),
        vmem((rows, genes), F32),
        vmem((cb, genes), F32),
        vmem((PLANE, rows, quarter), F32),
        vmem((PLANE, rows, quarter), F32),
        vmem((PLANE, rows, quarter), F32),
        vmem((spots, 3 * quarter), BF16),
        vmem((quarter, 3 * spots), BF16),
        vmem((quarter, 3 * genes), BF16),
        vmem((3, rows, LANES), F32),
        vmem((PLANE, 8, genes), F32),
        vmem((lines, 8, genes), F32),
        vmem((8, genes), F32),
        vmem((2, 8, rows), F32),
        vmem((3, rows, LANES), F32),
        vmem((PLANE, 8, rows), F32),
        vmem((spots, 3 * genes), BF16),
        vmem((3 * max(quarter, spots), max(FORWARD + BACKWARD)), BF16),
        vmem((PLANE, rows, BACKWARD[0]), F32),
        vmem((PLANE, rows, BACKWARD[0]), F32),
        vmem((PLANE, 8, rows), F32),
        vmem((spots, quarter), F32),
        vmem((PLANE, slide_rows, quarter), F32),
        vmem((PLANE, slide_rows, quarter), F32),
        vmem((PLANE, slide_rows, quarter), F32),
        vmem((PLANE, slide_rows, quarter), F32),
        vmem((2, rows, LANES), F32),
        vmem((PLANE, 8, LANES), F32),
        vmem((lines, 8, LANES), F32),
        dma((2 * slides + 4,)),
        dma((chunks,)),
        dma((chunks,)),
        dma((chunks,)),
        dma((chunks,)),
        dma((chunks,)),
        dma((chunks,)),
        dma((chunks,)),
        dma((chunks,)),
        dma,
        dma((PLANE,)),
        dma,
        dma((PLANE,)),
        dma,
        dma((PLANE,)),
        dma((chunks,)),
        dma((chunks, PLANE)),
        dma,
        dma((2, PLANE)),
        dma,
        dma((2, lines)),
        dma,
        dma,
        dma((turns,)),
        dma((turns, PLANE)),
        dma((turns,)),
        dma((turns, lines)),
        dma((turns,)),
        dma((turns, lines)),
        dma,
        dma((PLANE,)),
        dma,
        dma((PLANE,)),
        dma,
        dma((2,)),
        dma,
        dma,
        dma,
        dma((PLANE,)),
        dma,
        dma((lines,)),
        dma,
        dma((PLANE,)),
        dma,
        dma((PLANE,)),
        dma,
        dma((PLANE,)),
    ]
    for shape, widths in (
        ((quarter,), FORWARD),
        ((spots,), FORWARD),
        ((PLANE, rows), FORWARD),
        ((spots,), BACKWARD),
        ((quarter,), BACKWARD),
        ((quarter,), BACKWARD),
        ((quarter,), BACKWARD),
    ):
        scratch += [vmem(shape + (width,), F32) for width in widths]
    in_hbm = functools.partial(pltpu.with_memory_space_constraint, memory_space=pltpu.HBM)
    in_place = functools.partial(pltpu.with_memory_space_constraint, memory_space=pltpu.VMEM)
    results = pl.pallas_call(
        functools.partial(plane_kernel, lines, FORWARD, BACKWARD),
        out_shape=(
            vmem((rows, genes), F32),
            vmem((1, 1), F32),
            vmem((rows, cells), F32),
            vmem((cb, genes), F32),
        ),
        in_specs=[anywhere] * 6,
        out_specs=(in_vmem,) * 4,
        scratch_shapes=scratch,
        compiler_params=pltpu.CompilerParams(
            collective_id=0, has_side_effects=True, vmem_limit_bytes=48 * 1024 * 1024
        ),
    )(*map(in_hbm, (logits, expr, spatial, slide_spots, spot_cells, cell_prior.reshape(1, cells))))
    pred, loss, grad_logits, grad_expr = pl.pallas_call(
        deliver,
        out_shape=(
            jax.ShapeDtypeStruct((slides, slide_rows, genes), F32),
            jax.ShapeDtypeStruct((1, 1), F32),
            jax.ShapeDtypeStruct((slides, slide_rows, cells), F32),
            jax.ShapeDtypeStruct((cb, genes), F32),
        ),
        in_specs=[anywhere] * 4,
        out_specs=(anywhere,) * 4,
        scratch_shapes=[dma((2 * slides + 2,))],
        compiler_params=pltpu.CompilerParams(vmem_limit_bytes=4 * 1024 * 1024),
    )(*map(in_place, results))
    return pred, loss.reshape(()), grad_logits, grad_expr


def general_plan(logits, expr, spatial, slide_spots, spot_cells, cell_prior):
    place = lax.axis_index("spot")
    side = lax.axis_index("gene")
    rows_all = logits.shape[1]
    cell_rows = expr.shape[0]
    weights = cell_prior.astype(jnp.float32) / fixed_point
    gene_share = (place == 0).astype(jnp.float32)
    row_share = (side == 0).astype(jnp.float32)
    own_weights = lax.dynamic_slice_in_dim(weights, place * cell_rows, cell_rows, 0)
    expr_acc = jnp.zeros((cell_rows, expr.shape[1]), jnp.float32)
    loss_local = jnp.zeros((), jnp.float32)
    pred_list = []
    grad_list = []
    for slide in range(logits.shape[0]):
        logit_rows = logits[slide]
        counted = spot_cells[slide].astype(jnp.float32)
        target = spatial[slide]
        positions = place * rows_all + jnp.arange(rows_all, dtype=jnp.int32)
        valid = (positions < slide_spots[slide]).astype(jnp.float32)
        peak = jnp.max(logit_rows, axis=1, keepdims=True)
        raised = jnp.exp(logit_rows - peak)
        probs = raised / jnp.sum(raised, axis=1, keepdims=True)
        mass = jnp.dot(probs, weights, precision=lax.Precision.HIGHEST)
        blocks = lax.all_to_all(probs, "spot", split_axis=1, concat_axis=0, tiled=True)
        pred = lax.psum_scatter(
            jnp.dot(blocks, expr, precision=lax.Precision.HIGHEST),
            "spot",
            scatter_dimension=0,
            tiled=True,
        )
        gene_dot = jnp.sum(valid[:, None] * pred * target, axis=0)
        gene_pred = jnp.sum(valid[:, None] * pred * pred, axis=0)
        gene_true = jnp.sum(valid[:, None] * target * target, axis=0)
        mass_part = jnp.sum(valid * mass)
        kcell = valid * counted
        cell_part = jnp.sum(kcell)
        spot_dot = jnp.sum(pred * target, axis=1)
        spot_pred = jnp.sum(pred * pred, axis=1)
        spot_true = jnp.sum(target * target, axis=1)
        gene_dot, gene_pred, gene_true, mass_total, cell_total = lax.psum(
            (gene_dot, gene_pred, gene_true, mass_part, cell_part), "spot"
        )
        spot_dot, spot_pred, spot_true = lax.psum((spot_dot, spot_pred, spot_true), "gene")
        gene_inv = lax.rsqrt(gene_pred * gene_true + tiny)
        cos_gene = gene_dot * gene_inv
        spot_inv = lax.rsqrt(spot_pred * spot_true + tiny)
        cos_spot = spot_dot * spot_inv
        share = kcell / cell_total
        scale_count = slide_spots[slide].astype(jnp.float32)
        kl_part = jnp.sum(
            share * (jnp.log(counted) - jnp.log(cell_total) - jnp.log(mass) + jnp.log(mass_total))
        )
        loss_local = loss_local - gene_share * jnp.sum(cos_gene)
        loss_local = loss_local + row_share * (scale_count * kl_part - jnp.sum(valid * cos_spot))
        gene_back = cos_gene * gene_true / (gene_pred * gene_true + tiny)
        spot_back = cos_spot * spot_true / (spot_pred * spot_true + tiny)
        dpred = -valid[:, None] * (
            target * (gene_inv[None, :] + spot_inv[:, None])
            - pred * gene_back[None, :]
            - pred * spot_back[:, None]
        )
        dmass = scale_count * valid * (1.0 / mass_total - share / mass)
        pred_list.append(pred)
        grads_full, mass_full = (
            lax.all_gather(dpred, "spot", axis=0, tiled=True),
            lax.all_gather(dmass, "spot", axis=0, tiled=True),
        )
        dprob_cells = jnp.dot(grads_full, expr.T, precision=lax.Precision.HIGHEST)
        dprob_cells = lax.psum(dprob_cells, "gene")
        expr_acc = expr_acc + lax.dot_general(
            blocks, grads_full, (((0,), (0,)), ((), ())), precision=lax.Precision.HIGHEST
        )
        dprob_cells = dprob_cells + mass_full[:, None] * own_weights[None, :]
        dprob_rows = lax.all_to_all(dprob_cells, "spot", split_axis=0, concat_axis=1, tiled=True)
        inner = jnp.sum(probs * dprob_rows, axis=1, keepdims=True)
        dlogit = probs * (dprob_rows - inner)
        grad_list.append(dlogit)
    loss = lax.psum(loss_local, ("spot", "gene"))
    return (jnp.stack(pred_list), loss, jnp.stack(grad_list), expr_acc)


def solution(mesh):
    places = mesh.shape["spot"]

    def on_device(logits, expr, spatial, slide_spots, spot_cells, cell_prior):
        if places == PLANE * PLANE and mesh.shape["gene"] == 2 and expr.shape[1] == sum(FORWARD):
            return plane_call(
                logits, expr, spatial, slide_spots, spot_cells, cell_prior, places // PLANE
            )
        return general_plan(logits, expr, spatial, slide_spots, spot_cells, cell_prior)

    in_specs = (
        P(None, "spot", None),
        P("spot", "gene"),
        P(None, "spot", "gene"),
        P(),
        P(None, "spot"),
        P(),
    )
    out_specs = (P(None, "spot", "gene"), P(), P(None, "spot", None), P("spot", "gene"))
    return jax.shard_map(
        on_device, mesh=mesh, in_specs=in_specs, out_specs=out_specs, check_vma=False
    )
```

```python
import functools

import jax
import jax.numpy as jnp
from jax import lax
from jax.experimental import pallas as pl
from jax.experimental.pallas import tpu as pltpu
from jax.sharding import PartitionSpec as P

tiny = 1e-06
fixed_point = 16384.0
F32 = jnp.float32
BF16 = jnp.bfloat16
MESH = pl.DeviceIdType.MESH

PLANE = 4
LANES = 128
STEP_ROWS = 16
BLOCK = 32
TALL = 256
FORWARD = (128, 256, 256, 128, 128, 128)
BACKWARD = (128, 128, 256, 256, 256)
SPLIT = 2
LEAD = 2
NEAR_LEAD = 3
EARLY = 3
STEPS = (
    ("far", 0),
    ("far", 1),
    ("near", 0),
    ("share",),
    ("far", 2),
    ("far", 3),
    ("take",),
    ("whole", 0),
    ("near", 1),
    ("product", 0),
    ("sum", 0),
    ("whole", 1),
    ("near", 2),
    ("product", 1),
    ("whole", 2),
    ("product", 2),
    ("whole", 3),
    ("near", 3),
    ("product", 3),
    ("far", 4),
    ("whole", 4),
    ("near", 4),
    ("product", 4),
    ("sum", 1),
    ("turn", 0),
    ("far", 5),
    ("whole", 5),
    ("near", 5),
    ("product", 5),
    ("sum", 2),
    ("plane", 0),
    ("turn", 1),
    ("sum", 3),
    ("line", 0),
    ("sum", 4),
    ("sum", 5),
    ("cores",),
    ("plane", 1),
    ("genes", 0),
    ("spots",),
    ("grad", 0),
    ("grad", 1),
    ("grad", 2),
    ("line", 1),
    ("backward", 0),
    ("backward", 1),
    ("add_near", 0),
    ("genes", 1),
    ("grad", 3),
    ("backward", 2),
    ("probs", 0),
    ("add_far", 0),
    ("probs", 1),
    ("expr", 0),
    ("grad", 4),
    ("add_near", 1),
    ("probs", 2),
    ("terms",),
    ("backward", 3),
    ("probs", 3),
    ("add_near", 2),
    ("backward", 4),
    ("add_far", 1),
    ("probs", 4),
    ("exchange",),
    ("add_near", 3),
    ("add_far", 2),
    ("left",),
    ("return",),
    ("loss",),
    ("add_far", 3),
    ("expr", 1),
    ("add_near", 4),
    ("add_far", 4),
    ("logits",),
    ("expr", 2),
    ("expr", 3),
    ("expr", 4),
)


def halves(value):
    high = value.astype(BF16)
    return high, (value - high.astype(F32)).astype(BF16)


def threefold(value):
    high, low = halves(value)
    return jnp.concatenate([high, high, low], axis=1)


def product(a, b, contract):
    return lax.dot_general(a, b, (contract, ((), ())), preferred_element_type=F32)


def plane_kernel(lines, forward_widths, backward_widths, *refs):
    chunks, turns = len(forward_widths), len(backward_widths)
    (
        (logits_ref, expr_ref, spatial_ref, count_in, cells_in, prior_in),
        (pr, loss_ref, glog, ge),
        (count_ref, cells_ref, prior_ref, lg, lq, tg, ex, pq, ab, af, probs_3, turned_3, expr_3, sacc, s1, s2, gv, ss, rowv, rs),
        (grad_3, factor, t0, p0, vr, fs, fx, fy, fz, fr, inn, l1, l2),
        (loc, ou_s, ou_r, od_s, od_r, fu_s, fu_r, fd_s, fd_r, a_s, a_r, a2_s, a2_r, r_s, r_r),
        (c_s, c_r, s1_s, s1_r, s2_s, s2_r, ss_s, ss_r, d_s, d_r, ru_s, ru_r, rd_s, rd_r),
        (f_s, f_r, fx_s, fx_r, go_s, go_r, in_s, in_r, l1_s, l1_r, l2_s, l2_r, t0_s, t0_r, p0_s, p0_r, vr_s, vr_r),
        bb,
        cs,
        cr,
        ds,
        es,
        ru,
        rd,
    ) = grouped(refs, (6, 4, 20, 13, 15, 14, 18, chunks, chunks, chunks, turns, turns, turns, turns))
    place = lax.axis_index("spot")
    core = lax.axis_index("gene")
    z = place // PLANE
    q = place % PLANE
    col, row = q % 2, q // 2
    mates = ((1 - row) * 2 + 1 - col, row * 2 + 1 - col, (1 - row) * 2 + col)
    others = tuple((z + step) % lines for step in range(1, lines))
    up, down = (place + PLANE, core), (place - PLANE, core)
    sibling = (place, 1 - core)
    slides, slide_rows = logits_ref.shape[0], logits_ref.shape[1]
    rows = slides * slide_rows
    cb = expr_ref.shape[0]
    genes = expr_ref.shape[1]
    last = lines - 1

    def mate(p):
        return (z * PLANE + p, core)

    def send(src, dst, send_sem, recv_sem, device):
        copy = pltpu.make_async_remote_copy(
            src_ref=src, dst_ref=dst, send_sem=send_sem, recv_sem=recv_sem, device_id=device, device_id_type=MESH
        )
        copy.start()

    def arrived(dst, recv_sem):
        pltpu.make_async_copy(dst, dst, recv_sem).wait()

    sent = arrived

    def cols(k):
        return pl.ds(sum(forward_widths[:k]), forward_widths[k])

    def turn_cols(k):
        return pl.ds(sum(backward_widths[:k]), backward_widths[k])

    def block(index):
        return pl.ds(pl.multiple_of(index * cb, cb), cb)

    def share(index):
        return pl.ds(pl.multiple_of(index * rows, rows), rows)

    def half(index):
        return pl.ds(pl.multiple_of(index * slide_rows, slide_rows), slide_rows)

    small = ((prior_in, prior_ref), (count_in, count_ref), (cells_in, cells_ref))
    pltpu.make_async_copy(expr_ref, ex, loc.at[2 * slides]).start()
    for m in range(slides):
        pltpu.make_async_copy(logits_ref.at[m], lg.at[half(m)], loc.at[m]).start()
    for at, (src, dst) in enumerate(small):
        pltpu.make_async_copy(src, dst, loc.at[2 * slides + 1 + at]).start()
    for m in range(slides):
        pltpu.make_async_copy(spatial_ref.at[m], tg.at[half(m)], loc.at[slides + m]).start()

    barrier = pltpu.get_barrier_semaphore()
    for p in mates:
        pl.semaphore_signal(barrier, inc=1, device_id=mate(p), device_id_type=MESH)
    for o in others:
        pl.semaphore_signal(barrier, inc=1, device_id=(o * PLANE + q, core), device_id_type=MESH)
    pl.semaphore_signal(barrier, inc=1, device_id=sibling, device_id_type=MESH)
    pltpu.make_async_copy(expr_ref, ex, loc.at[2 * slides]).wait()
    for k in range(chunks):
        bb[k][block(z), :] = ex[:, cols(k)]
    for m in range(slides):
        pltpu.make_async_copy(logits_ref.at[m], lg.at[half(m)], loc.at[m]).wait()
    for p in range(PLANE):
        for line in range(lines):
            lq[p, :, pl.ds(line * cb, cb)] = lg[half(core), pl.ds((line * PLANE + p) * cb, cb)]
    pl.semaphore_wait(barrier, len(mates) + len(others) + 1)

    def own_up(k):
        here = bb[k].at[block(z)]
        send(here, here, ou_s.at[k], ou_r.at[k], up)

    def own_down(k):
        here = bb[k].at[block(z)]
        send(here, here, od_s.at[k], od_r.at[k], down)

    def low(at):
        return 2 * at < lines

    for at in range(lines):

        @pl.when(z == at)
        def _():
            for k in range(chunks):
                if at < last and (at == 0 or k < (LEAD if low(at) else NEAR_LEAD)):
                    own_up(k)
                if at > 0 and (at == last or k < (NEAR_LEAD if low(at) else LEAD)):
                    own_down(k)

    for p in mates:
        send(lq.at[p], ab.at[q, half(core)], a_s, a_r.at[q], mate(p))

    def from_below(k, at):
        arrived(bb[k].at[pl.ds((at - 1) * cb, cb)], ou_r.at[k])
        if at > 1:
            arrived(bb[k].at[pl.ds(0, (at - 1) * cb)], fu_r.at[k])

    def from_above(k, at):
        arrived(bb[k].at[pl.ds((at + 1) * cb, cb)], od_r.at[k])
        if at < last - 1:
            arrived(bb[k].at[pl.ds((at + 2) * cb, (last - 1 - at) * cb)], fd_r.at[k])

    def upward(k, at):
        from_below(k, at)
        here = bb[k].at[pl.ds(0, at * cb)]
        send(here, here, fu_s.at[k], fu_r.at[k], up)

    def downward(k, at):
        from_above(k, at)
        here = bb[k].at[pl.ds((at + 1) * cb, (last - at) * cb)]
        send(here, here, fd_s.at[k], fd_r.at[k], down)

    def forward_far(k):
        for at in range(1, last):

            @pl.when(z == at)
            def _():
                (upward if low(at) else downward)(k, at)
                if k + LEAD < chunks:
                    (own_up if low(at) else own_down)(k + LEAD)

    def forward_near(k):
        for at in range(1, last):

            @pl.when(z == at)
            def _():
                (downward if low(at) else upward)(k, at)
                if k + NEAR_LEAD < chunks:
                    (own_down if low(at) else own_up)(k + NEAR_LEAD)

    def gathered(k):
        @pl.when(z == 0)
        def _():
            from_above(k, 0)

        @pl.when(z == last)
        def _():
            from_below(k, last)

    for at, (src, dst) in enumerate(small):
        pltpu.make_async_copy(src, dst, loc.at[2 * slides + 1 + at]).wait()
    weights = prior_ref[...].astype(F32) / fixed_point

    @pl.loop(0, rows // STEP_ROWS)
    def _(step):
        at = pl.ds(pl.multiple_of(step * STEP_ROWS, STEP_ROWS), STEP_ROWS)
        value = lg[at, :]
        peak = jnp.max(value, axis=1, keepdims=True)
        raised = jnp.exp(value - peak)
        scale = 1.0 / jnp.sum(raised, axis=1, keepdims=True)
        probs = raised * scale
        mass_rows = jnp.sum(probs * weights, axis=1, keepdims=True)
        rowv[0, at, :] = jnp.broadcast_to(mass_rows, (STEP_ROWS, LANES))
        rowv[1, at, :] = jnp.broadcast_to(peak, (STEP_ROWS, LANES))
        rowv[2, at, :] = jnp.broadcast_to(scale, (STEP_ROWS, LANES))
        for p in range(PLANE):
            for line in range(lines):
                at_cells = (line * PLANE + p) * cb
                pq[p, at, pl.ds(line * cb, cb)] = probs[:, at_cells : at_cells + cb]

    wide = lax.broadcasted_iota(jnp.int32, (rows, LANES), 1)
    rs[q] = jnp.where(wide == 0, rowv[1], rowv[2]).T[0:8]
    for p in mates:
        send(rs.at[q], rs.at[q], r_s, r_r.at[q], mate(p))

    rid = lax.broadcasted_iota(jnp.int32, (rows, 1), 0)
    first = rid < slide_rows
    position = place * slide_rows + jnp.where(first, rid, rid - slide_rows)
    count = jnp.where(first, count_ref[0], count_ref[1])
    valid = (position < count).astype(F32)
    scale_count = count.astype(F32)
    square = (slide_rows, slide_rows)
    eye = lax.broadcasted_iota(jnp.int32, square, 0) == lax.broadcasted_iota(jnp.int32, square, 1)
    counted = jnp.concatenate(
        [
            jnp.sum(jnp.where(eye, cells_ref[m : m + 1, :].astype(F32), 0.0), axis=1, keepdims=True)
            for m in range(slides)
        ],
        axis=0,
    )
    mass = rowv[0, :, 0:1]
    kcell = valid * counted

    def by_slide(value):
        return [jnp.sum(value[m * slide_rows : (m + 1) * slide_rows], axis=0, keepdims=True) for m in range(slides)]

    mass_parts = by_slide(valid * mass)
    cell_parts = by_slide(kcell)
    lane = lax.broadcasted_iota(jnp.int32, (1, LANES), 1)
    scalars = jnp.zeros((1, LANES), F32)
    for at, value in enumerate(mass_parts + cell_parts):
        scalars = jnp.where(lane == at, value, scalars)
    for m in range(slides):
        pltpu.make_async_copy(spatial_ref.at[m], tg.at[half(m)], loc.at[slides + m]).wait()

    head = backward_widths[0]
    t0[q] = tg[:, 0:head]
    for p in mates:
        send(t0.at[q], t0.at[q], t0_s, t0_r.at[q], mate(p))
    sacc[...] = jnp.zeros_like(sacc)
    s1[q, 3 * slides :, :] = jnp.zeros((8 - 3 * slides, genes), F32)
    s1[q, 3 * slides : 3 * slides + 1, 0:LANES] = scalars

    def share_logits():
        for p in (mates[1], mates[2], mates[0]):
            here = ab.at[p, half(core)]
            arrived(here, a_r.at[p])
            send(here, here, a2_s, a2_r.at[p], sibling)

    def lay_probs(p, at, value):
        af[p, at, :] = value
        there = pl.ds(pl.multiple_of(p * rows + at.start, BLOCK), BLOCK)
        probs_3[there, :] = threefold(value)

    def take_probs():
        in_blocks(0, rows, lambda at: lay_probs(q, at, pq[q, at, :]))
        for p in (mates[1], mates[2], mates[0]):
            arrived(rs.at[p], r_r.at[p])
            arrived(ab.at[p, half(1 - core)], a2_r.at[p])
            rowv[1] = jnp.concatenate([rs[p].T, jnp.zeros((rows, LANES - 8), F32)], axis=1)

            def take(at):
                probs = jnp.exp(ab[p, at, :] - rowv[1, at, 0:1]) * rowv[1, at, 1:2]
                lay_probs(p, at, probs)

            in_blocks(0, rows, take)

    def transpose(part):
        @pl.loop(0, PLANE // 2)
        def _(step):
            p = part * (PLANE // 2) + step
            high, low_part = halves(af[p].T)
            for third, value in enumerate((high, high, low_part)):
                turned_3[:, pl.ds(pl.multiple_of(third * PLANE * rows + p * rows, rows), rows)] = value

    def in_blocks(start, count, body):
        @pl.loop(0, count // BLOCK)
        def _(step):
            body(pl.ds(pl.multiple_of(start + step * BLOCK, BLOCK), BLOCK))

    quarter = lines * cb

    def lay_factor(at, length, width, value):
        high, low_part = halves(value)
        for third, part in enumerate((high, low_part, high)):
            here = pl.ds(pl.multiple_of(third * length + at.start, BLOCK), BLOCK)
            factor[here, 0:width] = part

    def keep_expr(k, at, value):
        start = sum(forward_widths[:k])
        for turn in range(turns):
            origin, width = sum(backward_widths[:turn]), backward_widths[turn]
            lo, hi = max(start, origin), min(start + forward_widths[k], origin + width)
            if lo < hi:
                high, low_part = halves(value[:, lo - start : hi - start])
                for third, part in enumerate((high, low_part, high)):
                    expr_3[at, pl.ds(3 * origin + third * width + lo - origin, hi - lo)] = part

    def three_turn_cols(k):
        return pl.ds(3 * sum(backward_widths[:k]), 3 * backward_widths[k])

    def forward_product(k):
        width = forward_widths[k]

        def lay(at):
            value = bb[k][at, :]
            lay_factor(at, quarter, width, value)
            keep_expr(k, at, value)

        in_blocks(0, quarter, lay)
        if k < chunks - 1:

            @pl.loop(0, PLANE * rows // TALL)
            def _(step):
                tall = pl.ds(pl.multiple_of(step * TALL, TALL), TALL)
                cs[k][tall, :] = product(probs_3[tall, :], factor[0 : 3 * quarter, 0:width], ((1,), (0,)))

            for p in mates:
                pass_pred(k, p)
        else:
            for side, served in ((1 - row, (mates[0], mates[2])), (row, (mates[1],))):
                pair = pl.ds(pl.multiple_of(2 * side * rows, 2 * rows), 2 * rows)
                cs[k][pair, :] = product(probs_3[pair, :], factor[0 : 3 * quarter, 0:width], ((1,), (0,)))
                for p in served:
                    pass_pred(k, p)

    def pass_pred(k, p):
        send(cs[k].at[share(p)], cr[k].at[q], c_s.at[k], c_r.at[k, q], mate(p))

    def finish_pred(k):
        total = cs[k][share(q), :]
        for p in mates:
            arrived(cr[k].at[p], c_r.at[k, p])
            total = total + cr[k][p]
        pr[:, cols(k)] = total
        if k == 0:
            p0[q] = total[:, 0:head]
            for p in mates:
                send(p0.at[q], p0.at[q], p0_s, p0_r.at[q], mate(p))
        truth = tg[:, cols(k)]
        for at, value in enumerate((total * truth, total * total, truth * truth)):
            sacc[at] += lane_groups(value)
        kept = valid * total
        stats = by_slide(kept * truth) + by_slide(kept * total) + by_slide(valid * truth * truth)
        s1[q, 0 : 3 * slides, cols(k)] = jnp.concatenate(stats, axis=0)

    early = sum(forward_widths[:EARLY])
    parts = (pl.ds(0, early), pl.ds(early, genes - early))

    def sum_plane(at):
        for p in mates:
            send(s1.at[q, :, parts[at]], s1.at[q, :, parts[at]], s1_s, s1_r.at[at, q], mate(p))

    def sum_line(at):
        for p in mates:
            arrived(s1.at[p, :, parts[at]], s1_r.at[at, p])
        s2[z, :, parts[at]] = (s1[0, :, parts[at]] + s1[1, :, parts[at]]) + (s1[2, :, parts[at]] + s1[3, :, parts[at]])
        for o in others:
            send(s2.at[z, :, parts[at]], s2.at[z, :, parts[at]], s2_s, s2_r.at[at, z], (o * PLANE + q, core))

    kept = {}

    def finish_genes(at):
        for o in others:
            arrived(s2.at[o, :, parts[at]], s2_r.at[at, o])
        total = s2[0, :, parts[at]]
        for line in range(1, lines):
            total = total + s2[line, :, parts[at]]
        gene_dot, gene_pred, gene_true = total[0:2], total[2:4], total[4:6]
        gene_inv = lax.rsqrt(gene_pred * gene_true + tiny)
        cos_gene = gene_dot * gene_inv
        gv[0:2, parts[at]] = gene_inv
        gv[2:4, parts[at]] = cos_gene * gene_true / (gene_pred * gene_true + tiny)
        kept["genes", at] = jnp.sum(jnp.sum(cos_gene, axis=1, keepdims=True), axis=0, keepdims=True)
        if at == 0:
            kept["mass"] = jnp.where(first, total[6:7, 0:1], total[6:7, 1:2])
            kept["cells"] = jnp.where(first, total[6:7, 2:3], total[6:7, 3:4])

    def sum_cores():
        sums = [jnp.sum(sacc[at], axis=1, keepdims=True) for at in range(3)]
        ss[core] = jnp.where(wide == 0, sums[0], jnp.where(wide == 1, sums[1], sums[2])).T[0:8]
        send(ss.at[core], ss.at[core], ss_s, ss_r, sibling)

    def finish_spots():
        lane_id = lax.broadcasted_iota(jnp.int32, (1, rows), 1)
        first_lane = lane_id < slide_rows
        lane_position = place * slide_rows + jnp.where(first_lane, lane_id, lane_id - slide_rows)
        lane_valid = (lane_position < jnp.where(first_lane, count_ref[0], count_ref[1])).astype(F32)
        arrived(ss.at[1 - core], ss_r)
        spot = ss[0] + ss[1]
        spot_dot, spot_pred, spot_true = spot[0:1], spot[1:2], spot[2:3]
        spot_inv = lax.rsqrt(spot_pred * spot_true + tiny)
        cos_spot = spot_dot * spot_inv
        spot_back = cos_spot * spot_true / (spot_pred * spot_true + tiny)
        kept["cos"] = jnp.sum(lane_valid * cos_spot, axis=1, keepdims=True)
        vectors = [lane_valid * spot_inv, lane_valid * spot_back, lane_valid, jnp.zeros((5, rows), F32)]
        vr[q] = jnp.concatenate(vectors, axis=0)
        sacc[0] = jnp.zeros_like(sacc[0])

    def gradient(truth, guess, by_row, k):
        pieces = []
        for m in range(slides):
            lo, hi = m * slide_rows, (m + 1) * slide_rows
            inverse, back = gv[m : m + 1, turn_cols(k)], gv[2 + m : 3 + m, turn_cols(k)]
            spot_inv, spot_back, spot_valid = by_row[lo:hi, 0:1], by_row[lo:hi, 1:2], by_row[lo:hi, 2:3]
            pieces.append(
                guess[lo:hi] * (spot_valid * back + spot_back) - truth[lo:hi] * (spot_valid * inverse + spot_inv)
            )
        return jnp.concatenate(pieces, axis=0)

    def head_gradient():
        for p in mates:
            arrived(t0.at[p], t0_r.at[p])
            arrived(p0.at[p], p0_r.at[p])
            arrived(vr.at[p], vr_r.at[p])
        for p in range(PLANE):
            ds[0][share(p), :] = gradient(t0[p], p0[p], vr[p].T, 0)
        sacc[0] += lane_groups(ds[0][share(q), :] * p0[q])

    def send_grad(k):
        if k == 0:
            for p in mates:
                send(vr.at[q], vr.at[q], vr_s, vr_r.at[q], mate(p))
            kept["by_row"] = vr[q].T
            return
        grad = gradient(tg[:, turn_cols(k)], pr[:, turn_cols(k)], kept["by_row"], k)
        here = ds[k].at[share(q)]
        here[...] = grad
        for p in mates:
            send(here, here, d_s.at[k], d_r.at[k, q], mate(p))
        sacc[0] += lane_groups(grad * pr[:, turn_cols(k)])

    def send_terms():
        mass_total, cell_total = kept["mass"], kept["cells"]
        portion = kcell / cell_total
        kl_rows = portion * (jnp.log(counted) - jnp.log(cell_total) - jnp.log(mass) + jnp.log(mass_total))
        dmass = scale_count * valid * (1.0 / mass_total - portion / mass)
        terms = jnp.sum(scale_count * kl_rows, axis=0, keepdims=True) - kept["cos"]
        l1[q] = jnp.broadcast_to(terms, (8, LANES))
        for p in mates:
            send(l1.at[q], l1.at[q], l1_s, l1_r.at[q], mate(p))
        inner = jnp.sum(sacc[0], axis=1, keepdims=True)
        inn[core] = jnp.where(wide == 0, inner, kept["genes", 0] + kept["genes", 1])
        send(inn.at[core], inn.at[core], in_s, in_r, sibling)
        rowv[1] = jnp.broadcast_to(dmass, (rows, LANES))

    middle = lines // 2

    def backward_product(k):
        if k == 0:
            head_gradient()
        else:
            for p in mates:
                arrived(ds[k].at[share(p)], d_r.at[k, p])
        width, spots = backward_widths[k], PLANE * rows

        def lay(at):
            value = ds[k][at, :]
            lay_factor(at, spots, width, value)
            grad_3[at, three_turn_cols(k)] = threefold(value)

        in_blocks(0, spots, lay)
        if not halved(k):

            @pl.loop(0, quarter // TALL)
            def _(step):
                tall = pl.ds(pl.multiple_of(step * TALL, TALL), TALL)
                es[k][tall, :] = product(turned_3[tall, :], factor[0 : 3 * spots, 0:width], ((1,), (0,)))

        for turn in range(2):
            if halved(k):
                side = (1 - z // middle) if turn == 0 else z // middle
                pair = pl.ds(pl.multiple_of(side * middle * cb, middle * cb), middle * cb)
                es[k][pair, :] = product(turned_3[pair, :], factor[0 : 3 * spots, 0:width], ((1,), (0,)))

            @pl.when(z == 0)
            def _():
                if halved(k):
                    pass_up(k, middle if turn == 0 else 1, middle if turn == 0 else middle - 1, turn)
                elif whole(k):
                    if turn == 0:
                        pass_up(k, 1, last, 0)
                elif turn == 0:
                    for line in range(last, 0, -1):
                        pass_up(k, line, 1, line)

            @pl.when(z == last)
            def _():
                if halved(k):
                    pass_down(k, 0 if turn == 0 else middle, middle if turn == 0 else middle - 1, turn)
                elif whole(k):
                    if turn == 0:
                        pass_down(k, 0, last, 0)
                elif turn == 0:
                    for line in range(last):
                        pass_down(k, line, 1, line)

    def halved(k):
        return k == 0

    def whole(k):
        return 0 < k < turns - SPLIT

    def pass_up(k, line, count, slot):
        here = pl.ds(line * cb, count * cb)
        send(es[k].at[here], ru[k].at[here], ru_s.at[k], ru_r.at[k, slot], up)

    def pass_down(k, line, count, slot):
        here = pl.ds(line * cb, count * cb)
        send(es[k].at[here], rd[k].at[here], rd_s.at[k], rd_r.at[k, slot], down)

    def take_up(k, line, count, slot):
        arrived(ru[k].at[pl.ds(line * cb, count * cb)], ru_r.at[k, slot])

    def take_down(k, line, count, slot):
        arrived(rd[k].at[pl.ds(line * cb, count * cb)], rd_r.at[k, slot])

    def add_up(k, line, count):
        def add(at):
            es[k][at, :] += ru[k][at, :]

        in_blocks(line * cb, count * cb, add)

    def add_down(k, line, count):
        def add(at):
            es[k][at, :] += rd[k][at, :]

        in_blocks(line * cb, count * cb, add)

    def rising(k, at):
        if halved(k) or whole(k):
            start = middle if halved(k) else at
            take_up(k, start, lines - start, 0)
            above = max(at + 1, start)
            add_up(k, above, lines - above)
            pass_up(k, above, lines - above, 0)
        else:
            for line in range(last, at, -1):
                take_up(k, line, 1, line)
                add_up(k, line, 1)
                pass_up(k, line, 1, line)

    def falling(k, at):
        if halved(k) or whole(k):
            end = middle if halved(k) else at + 1
            take_down(k, 0, end, 0)
            below = min(at, end)
            add_down(k, 0, below)
            pass_down(k, 0, below, 0)
        else:
            for line in range(at):
                take_down(k, line, 1, line)
                add_down(k, line, 1)
                pass_down(k, line, 1, line)

    def add_near(k):
        for at in range(1, last):

            @pl.when(z == at)
            def _():
                (rising if low(at) else falling)(k, at)

    def add_far(k):
        for at in range(1, last):

            @pl.when(z == at)
            def _():
                (falling if low(at) else rising)(k, at)

    def finish_expr(k):
        for at in range(lines):

            @pl.when(z == at)
            def _():
                if at > 0:
                    if halved(k) and at < middle:
                        take_up(k, at, 1, 1)
                    elif at == last and (halved(k) or whole(k)):
                        take_up(k, at, 1, 0)
                    elif not halved(k) and not whole(k):
                        take_up(k, at, 1, at)
                if at < last:
                    if halved(k) and at >= middle:
                        take_down(k, at, 1, 1)
                    elif at == 0 and (halved(k) or whole(k)):
                        take_down(k, at, 1, 0)
                    elif not halved(k) and not whole(k):
                        take_down(k, at, 1, at)

        from_low, from_high = z > 0, z < last

        @pl.loop(0, cb // BLOCK)
        def _(step):
            here = pl.ds(pl.multiple_of(step * BLOCK, BLOCK), BLOCK)
            own = pl.ds(pl.multiple_of(z * cb + step * BLOCK, BLOCK), BLOCK)
            total = es[k][own, :]
            total = total + jnp.where(from_low, ru[k][own, :], 0.0)
            ge[here, turn_cols(k)] = total + jnp.where(from_high, rd[k][own, :], 0.0)

    def probs_gradient(k):
        at = three_turn_cols(k)

        @pl.loop(0, PLANE * rows // TALL)
        def _(step):
            tall = pl.ds(pl.multiple_of(step * TALL, TALL), TALL)
            part = product(grad_3[tall, at], expr_3[:, at], ((1,), (1,)))
            if k == 0:
                fs[tall, :] = part
            else:
                fs[tall, :] += part

    def slide_of(p, m):
        return pl.ds(pl.multiple_of(p * rows + m * slide_rows, slide_rows), slide_rows)

    def sum_probs_cores():
        for p in mates + (q,):
            fx[p] = fs[slide_of(p, 1 - core), :]
            send(fx.at[p], fy.at[p], fx_s, fx_r.at[p], sibling)

    def return_probs():
        for p in mates:
            arrived(fy.at[p], fx_r.at[p])
            fz[p] = fs[slide_of(p, core), :] + fy[p]
            send(fz.at[p], fr.at[q], f_s, f_r.at[q], mate(p))
        arrived(fy.at[q], fx_r.at[q])
        fr[q] = fs[slide_of(q, core), :] + fy[q]

    def pass_terms():
        for p in mates:
            arrived(l1.at[p], l1_r.at[p])
        l2[z] = (l1[0] + l1[1]) + (l1[2] + l1[3])
        for o in others:
            send(l2.at[z], l2.at[z], l2_s, l2_r.at[z], (o * PLANE + q, core))

    def part_of(slide, m):
        start = slide * slide_rows + m * (slide_rows // 2)
        return pl.ds(pl.multiple_of(start, slide_rows // 2), slide_rows // 2)

    def finish_logits():
        arrived(inn.at[1 - core], in_r)
        rowv[2] = (inn[0] + inn[1]) + rowv[1] * rowv[0]
        for p in mates:
            arrived(fr.at[p], f_r.at[p])
        for m in range(2):

            @pl.loop(0, slide_rows // STEP_ROWS // 2)
            def _(step):
                row_at = (m * (slide_rows // STEP_ROWS // 2) + step) * STEP_ROWS
                at = pl.ds(pl.multiple_of(row_at, STEP_ROWS), STEP_ROWS)
                whole_at = pl.ds(pl.multiple_of(core * slide_rows + row_at, STEP_ROWS), STEP_ROWS)
                by_mass, total_inner = rowv[1, whole_at, 0:1], rowv[2, whole_at, 0:1]
                for p in range(PLANE):
                    for line in range(lines):
                        here, there = pl.ds(line * cb, cb), (line * PLANE + p) * cb
                        grad = fr[p, at, here] + by_mass * weights[:, there : there + cb]
                        glog[whole_at, pl.ds(there, cb)] = pq[p, whole_at, here] * (grad - total_inner)

            here = part_of(core, m)
            send(glog.at[here], glog.at[here], go_s, go_r.at[m], sibling)

    def forward_left():
        for k in range(chunks):

            @pl.when(z < last)
            def _():
                sent(bb[k].at[block(z)], ou_s.at[k])

            @pl.when(z > 0)
            def _():
                sent(bb[k].at[block(z)], od_s.at[k])

            for at in range(1, last):

                @pl.when(z == at)
                def _():
                    sent(bb[k].at[pl.ds(0, at * cb)], fu_s.at[k])
                    sent(bb[k].at[pl.ds((at + 1) * cb, (last - at) * cb)], fd_s.at[k])

        three = pl.ds(0, len(mates))
        sent(ab.at[three, half(0)], a_s)
        sent(ab.at[three, half(0)], a2_s)
        sent(rs.at[three], r_s)
        sent(t0.at[three], t0_s)
        sent(p0.at[three], p0_s)
        for k in range(chunks):
            sent(cr[k].at[three], c_s.at[k])
        sent(s1.at[three], s1_s)
        sent(s2.at[pl.ds(0, last)], s2_s)
        sent(ss.at[0], ss_s)

    steps = {
        "far": forward_far,
        "near": forward_near,
        "share": share_logits,
        "take": take_probs,
        "whole": gathered,
        "product": forward_product,
        "sum": finish_pred,
        "turn": transpose,
        "plane": sum_plane,
        "line": sum_line,
        "genes": finish_genes,
        "cores": sum_cores,
        "spots": finish_spots,
        "grad": send_grad,
        "terms": send_terms,
        "backward": backward_product,
        "probs": probs_gradient,
        "exchange": sum_probs_cores,
        "return": return_probs,
        "loss": pass_terms,
        "logits": finish_logits,
        "add_near": add_near,
        "add_far": add_far,
        "expr": finish_expr,
        "left": forward_left,
    }
    for name, *where in STEPS:
        steps[name](*where)

    for o in others:
        arrived(l2.at[o], l2_r.at[o])
    loss = l2[0]
    for line in range(1, lines):
        loss = loss + l2[line]
    loss_ref[...] = loss[0:1, 0:1] - (inn[0, 0:1, 1:2] + inn[1, 0:1, 1:2])
    for m in range(2):
        arrived(glog.at[part_of(1 - core, m)], go_r.at[m])

    for k in range(turns):
        for at in range(lines):

            @pl.when(z == at)
            def _():
                if at < last:
                    sent(es[k].at[pl.ds((at + 1) * cb, (last - at) * cb)], ru_s.at[k])
                if at > 0:
                    sent(es[k].at[pl.ds(0, at * cb)], rd_s.at[k])

    three = pl.ds(0, len(mates))
    for k in range(1, turns):
        sent(ds[k].at[pl.ds(0, len(mates) * rows)], d_s.at[k])
    sent(vr.at[three], vr_s)
    sent(inn.at[0], in_s)
    sent(l1.at[three], l1_s)
    sent(l2.at[pl.ds(0, last)], l2_s)
    sent(fr.at[three], f_s)
    sent(fx, fx_s)
    sent(glog.at[half(0)], go_s)


def lane_groups(value):
    parts = [value[:, at : at + LANES] for at in range(0, value.shape[1], LANES)]
    return functools.reduce(lambda a, b: a + b, parts)


def grouped(refs, sizes):
    at = 0
    for size in sizes:
        yield refs[at : at + size]
        at += size


def deliver(pred_in, loss_in, glog_in, gexp_in, pred_ref, loss_ref, glog_ref, gexp_ref, sems):
    slides, slide_rows = pred_ref.shape[0], pred_ref.shape[1]
    pairs = [(gexp_in, gexp_ref), (loss_in, loss_ref)]
    for m in range(slides):
        part = pl.ds(m * slide_rows, slide_rows)
        pairs += [(glog_in.at[part], glog_ref.at[m]), (pred_in.at[part], pred_ref.at[m])]
    copies = [pltpu.make_async_copy(src, dst, sems.at[at]) for at, (src, dst) in enumerate(pairs)]
    for copy in copies:
        copy.start()
    for copy in copies:
        copy.wait()


def plane_call(logits, expr, spatial, slide_spots, spot_cells, cell_prior, lines):
    slides, slide_rows, cells = logits.shape
    rows = slides * slide_rows
    cb, genes = expr.shape
    quarter = lines * cb
    spots = PLANE * rows
    chunks, turns = len(FORWARD), len(BACKWARD)
    dma = pltpu.SemaphoreType.DMA
    vmem = pltpu.VMEM
    anywhere = pl.BlockSpec(memory_space=pl.ANY)
    in_vmem = pl.BlockSpec(memory_space=pltpu.VMEM)
    scratch = [
        pltpu.SMEM((slides,), jnp.int32),
        vmem((slides, slide_rows), jnp.int32),
        vmem((1, cells), jnp.int32),
        vmem((rows, cells), F32),
        vmem((PLANE, slide_rows, quarter), F32),
        vmem((rows, genes), F32),
        vmem((cb, genes), F32),
        vmem((PLANE, rows, quarter), F32),
        vmem((PLANE, rows, quarter), F32),
        vmem((PLANE, rows, quarter), F32),
        vmem((spots, 3 * quarter), BF16),
        vmem((quarter, 3 * spots), BF16),
        vmem((quarter, 3 * genes), BF16),
        vmem((3, rows, LANES), F32),
        vmem((PLANE, 8, genes), F32),
        vmem((lines, 8, genes), F32),
        vmem((8, genes), F32),
        vmem((2, 8, rows), F32),
        vmem((3, rows, LANES), F32),
        vmem((PLANE, 8, rows), F32),
        vmem((spots, 3 * genes), BF16),
        vmem((3 * max(quarter, spots), max(FORWARD + BACKWARD)), BF16),
        vmem((PLANE, rows, BACKWARD[0]), F32),
        vmem((PLANE, rows, BACKWARD[0]), F32),
        vmem((PLANE, 8, rows), F32),
        vmem((spots, quarter), F32),
        vmem((PLANE, slide_rows, quarter), F32),
        vmem((PLANE, slide_rows, quarter), F32),
        vmem((PLANE, slide_rows, quarter), F32),
        vmem((PLANE, slide_rows, quarter), F32),
        vmem((2, rows, LANES), F32),
        vmem((PLANE, 8, LANES), F32),
        vmem((lines, 8, LANES), F32),
        dma((2 * slides + 4,)),
        dma((chunks,)),
        dma((chunks,)),
        dma((chunks,)),
        dma((chunks,)),
        dma((chunks,)),
        dma((chunks,)),
        dma((chunks,)),
        dma((chunks,)),
        dma,
        dma((PLANE,)),
        dma,
        dma((PLANE,)),
        dma,
        dma((PLANE,)),
        dma((chunks,)),
        dma((chunks, PLANE)),
        dma,
        dma((2, PLANE)),
        dma,
        dma((2, lines)),
        dma,
        dma,
        dma((turns,)),
        dma((turns, PLANE)),
        dma((turns,)),
        dma((turns, lines)),
        dma((turns,)),
        dma((turns, lines)),
        dma,
        dma((PLANE,)),
        dma,
        dma((PLANE,)),
        dma,
        dma((2,)),
        dma,
        dma,
        dma,
        dma((PLANE,)),
        dma,
        dma((lines,)),
        dma,
        dma((PLANE,)),
        dma,
        dma((PLANE,)),
        dma,
        dma((PLANE,)),
    ]
    for shape, widths in (
        ((quarter,), FORWARD),
        ((spots,), FORWARD),
        ((PLANE, rows), FORWARD),
        ((spots,), BACKWARD),
        ((quarter,), BACKWARD),
        ((quarter,), BACKWARD),
        ((quarter,), BACKWARD),
    ):
        scratch += [vmem(shape + (width,), F32) for width in widths]
    in_hbm = functools.partial(pltpu.with_memory_space_constraint, memory_space=pltpu.HBM)
    in_place = functools.partial(pltpu.with_memory_space_constraint, memory_space=pltpu.VMEM)
    results = pl.pallas_call(
        functools.partial(plane_kernel, lines, FORWARD, BACKWARD),
        out_shape=(
            vmem((rows, genes), F32),
            vmem((1, 1), F32),
            vmem((rows, cells), F32),
            vmem((cb, genes), F32),
        ),
        in_specs=[anywhere] * 6,
        out_specs=(in_vmem,) * 4,
        scratch_shapes=scratch,
        compiler_params=pltpu.CompilerParams(
            collective_id=0, has_side_effects=True, vmem_limit_bytes=48 * 1024 * 1024
        ),
    )(*map(in_hbm, (logits, expr, spatial, slide_spots, spot_cells, cell_prior.reshape(1, cells))))
    pred, loss, grad_logits, grad_expr = pl.pallas_call(
        deliver,
        out_shape=(
            jax.ShapeDtypeStruct((slides, slide_rows, genes), F32),
            jax.ShapeDtypeStruct((1, 1), F32),
            jax.ShapeDtypeStruct((slides, slide_rows, cells), F32),
            jax.ShapeDtypeStruct((cb, genes), F32),
        ),
        in_specs=[anywhere] * 4,
        out_specs=(anywhere,) * 4,
        scratch_shapes=[dma((2 * slides + 2,))],
        compiler_params=pltpu.CompilerParams(vmem_limit_bytes=4 * 1024 * 1024),
    )(*map(in_place, results))
    return pred, loss.reshape(()), grad_logits, grad_expr


def general_plan(logits, expr, spatial, slide_spots, spot_cells, cell_prior):
    place = lax.axis_index("spot")
    side = lax.axis_index("gene")
    rows_all = logits.shape[1]
    cell_rows = expr.shape[0]
    weights = cell_prior.astype(jnp.float32) / fixed_point
    gene_share = (place == 0).astype(jnp.float32)
    row_share = (side == 0).astype(jnp.float32)
    own_weights = lax.dynamic_slice_in_dim(weights, place * cell_rows, cell_rows, 0)
    expr_acc = jnp.zeros((cell_rows, expr.shape[1]), jnp.float32)
    loss_local = jnp.zeros((), jnp.float32)
    pred_list = []
    grad_list = []
    for slide in range(logits.shape[0]):
        logit_rows = logits[slide]
        counted = spot_cells[slide].astype(jnp.float32)
        target = spatial[slide]
        positions = place * rows_all + jnp.arange(rows_all, dtype=jnp.int32)
        valid = (positions < slide_spots[slide]).astype(jnp.float32)
        peak = jnp.max(logit_rows, axis=1, keepdims=True)
        raised = jnp.exp(logit_rows - peak)
        probs = raised / jnp.sum(raised, axis=1, keepdims=True)
        mass = jnp.dot(probs, weights, precision=lax.Precision.HIGHEST)
        blocks = lax.all_to_all(probs, "spot", split_axis=1, concat_axis=0, tiled=True)
        pred = lax.psum_scatter(
            jnp.dot(blocks, expr, precision=lax.Precision.HIGHEST),
            "spot",
            scatter_dimension=0,
            tiled=True,
        )
        gene_dot = jnp.sum(valid[:, None] * pred * target, axis=0)
        gene_pred = jnp.sum(valid[:, None] * pred * pred, axis=0)
        gene_true = jnp.sum(valid[:, None] * target * target, axis=0)
        mass_part = jnp.sum(valid * mass)
        kcell = valid * counted
        cell_part = jnp.sum(kcell)
        spot_dot = jnp.sum(pred * target, axis=1)
        spot_pred = jnp.sum(pred * pred, axis=1)
        spot_true = jnp.sum(target * target, axis=1)
        gene_dot, gene_pred, gene_true, mass_total, cell_total = lax.psum(
            (gene_dot, gene_pred, gene_true, mass_part, cell_part), "spot"
        )
        spot_dot, spot_pred, spot_true = lax.psum((spot_dot, spot_pred, spot_true), "gene")
        gene_inv = lax.rsqrt(gene_pred * gene_true + tiny)
        cos_gene = gene_dot * gene_inv
        spot_inv = lax.rsqrt(spot_pred * spot_true + tiny)
        cos_spot = spot_dot * spot_inv
        share = kcell / cell_total
        scale_count = slide_spots[slide].astype(jnp.float32)
        kl_part = jnp.sum(
            share * (jnp.log(counted) - jnp.log(cell_total) - jnp.log(mass) + jnp.log(mass_total))
        )
        loss_local = loss_local - gene_share * jnp.sum(cos_gene)
        loss_local = loss_local + row_share * (scale_count * kl_part - jnp.sum(valid * cos_spot))
        gene_back = cos_gene * gene_true / (gene_pred * gene_true + tiny)
        spot_back = cos_spot * spot_true / (spot_pred * spot_true + tiny)
        dpred = -valid[:, None] * (
            target * (gene_inv[None, :] + spot_inv[:, None])
            - pred * gene_back[None, :]
            - pred * spot_back[:, None]
        )
        dmass = scale_count * valid * (1.0 / mass_total - share / mass)
        pred_list.append(pred)
        grads_full, mass_full = (
            lax.all_gather(dpred, "spot", axis=0, tiled=True),
            lax.all_gather(dmass, "spot", axis=0, tiled=True),
        )
        dprob_cells = jnp.dot(grads_full, expr.T, precision=lax.Precision.HIGHEST)
        dprob_cells = lax.psum(dprob_cells, "gene")
        expr_acc = expr_acc + lax.dot_general(
            blocks, grads_full, (((0,), (0,)), ((), ())), precision=lax.Precision.HIGHEST
        )
        dprob_cells = dprob_cells + mass_full[:, None] * own_weights[None, :]
        dprob_rows = lax.all_to_all(dprob_cells, "spot", split_axis=0, concat_axis=1, tiled=True)
        inner = jnp.sum(probs * dprob_rows, axis=1, keepdims=True)
        dlogit = probs * (dprob_rows - inner)
        grad_list.append(dlogit)
    loss = lax.psum(loss_local, ("spot", "gene"))
    return (jnp.stack(pred_list), loss, jnp.stack(grad_list), expr_acc)


def solution(mesh):
    places = mesh.shape["spot"]

    def on_device(logits, expr, spatial, slide_spots, spot_cells, cell_prior):
        if places == PLANE * PLANE and mesh.shape["gene"] == 2 and expr.shape[1] == sum(FORWARD):
            return plane_call(
                logits, expr, spatial, slide_spots, spot_cells, cell_prior, places // PLANE
            )
        return general_plan(logits, expr, spatial, slide_spots, spot_cells, cell_prior)

    in_specs = (
        P(None, "spot", None),
        P("spot", "gene"),
        P(None, "spot", "gene"),
        P(),
        P(None, "spot"),
        P(),
    )
    out_specs = (P(None, "spot", "gene"), P(), P(None, "spot", None), P("spot", "gene"))
    return jax.shard_map(
        on_device, mesh=mesh, in_specs=in_specs, out_specs=out_specs, check_vma=False
    )
```

```python
import functools

import jax
import jax.numpy as jnp
from jax import lax
from jax.experimental import pallas as pl
from jax.experimental.pallas import tpu as pltpu
from jax.sharding import PartitionSpec as P

tiny = 1e-06
fixed_point = 16384.0
F32 = jnp.float32
BF16 = jnp.bfloat16
MESH = pl.DeviceIdType.MESH

PLANE = 4
LANES = 128
STEP_ROWS = 16
BLOCK = 32
TALL = 256
FORWARD = (128, 256, 256, 128, 128, 128)
BACKWARD = (128, 128, 256, 256, 256)
SPLIT = 2
LEAD = 1
NEAR_LEAD = 3
EARLY = 3
STEPS = (
    ("far", 0),
    ("far", 1),
    ("near", 0),
    ("share",),
    ("far", 2),
    ("far", 3),
    ("take",),
    ("whole", 0),
    ("near", 1),
    ("product", 0),
    ("sum", 0),
    ("whole", 1),
    ("near", 2),
    ("product", 1),
    ("whole", 2),
    ("product", 2),
    ("whole", 3),
    ("near", 3),
    ("product", 3),
    ("far", 4),
    ("whole", 4),
    ("near", 4),
    ("product", 4),
    ("sum", 1),
    ("turn", 0),
    ("far", 5),
    ("whole", 5),
    ("near", 5),
    ("product", 5),
    ("sum", 2),
    ("plane", 0),
    ("turn", 1),
    ("sum", 3),
    ("line", 0),
    ("sum", 4),
    ("sum", 5),
    ("plane", 1),
    ("cores",),
    ("genes", 0),
    ("spots",),
    ("grad", 0),
    ("grad", 1),
    ("grad", 2),
    ("line", 1),
    ("backward", 0),
    ("backward", 1),
    ("add_near", 0),
    ("genes", 1),
    ("grad", 3),
    ("backward", 2),
    ("probs", 0),
    ("add_far", 0),
    ("probs", 1),
    ("expr", 0),
    ("grad", 4),
    ("add_near", 1),
    ("probs", 2),
    ("terms",),
    ("backward", 3),
    ("probs", 3),
    ("add_near", 2),
    ("backward", 4),
    ("add_far", 1),
    ("probs", 4),
    ("exchange",),
    ("add_near", 3),
    ("add_far", 2),
    ("left",),
    ("return",),
    ("loss",),
    ("add_far", 3),
    ("expr", 1),
    ("add_near", 4),
    ("logits",),
    ("add_far", 4),
    ("expr", 2),
    ("expr", 3),
    ("expr", 4),
)


def halves(value):
    high = value.astype(BF16)
    return high, (value - high.astype(F32)).astype(BF16)


def threefold(value):
    high, low = halves(value)
    return jnp.concatenate([high, high, low], axis=1)


def product(a, b, contract):
    return lax.dot_general(a, b, (contract, ((), ())), preferred_element_type=F32)


def plane_kernel(lines, forward_widths, backward_widths, *refs):
    chunks, turns = len(forward_widths), len(backward_widths)
    (
        (logits_ref, expr_ref, spatial_ref, count_in, cells_in, prior_in),
        (pr, loss_ref, glog, ge),
        (count_ref, cells_ref, prior_ref, lg, lq, tg, ex, pq, ab, af, probs_3, turned_3, expr_3, sacc, s1, s2, gv, ss, rowv, rs),
        (grad_3, factor, t0, p0, vr, fs, fx, fy, fz, fr, inn, l1, l2),
        (loc, ou_s, ou_r, od_s, od_r, fu_s, fu_r, fd_s, fd_r, a_s, a_r, a2_s, a2_r, r_s, r_r),
        (c_s, c_r, s1_s, s1_r, s2_s, s2_r, ss_s, ss_r, d_s, d_r, ru_s, ru_r, rd_s, rd_r),
        (f_s, f_r, fx_s, fx_r, go_s, go_r, in_s, in_r, l1_s, l1_r, l2_s, l2_r, t0_s, t0_r, p0_s, p0_r, vr_s, vr_r),
        bb,
        cs,
        cr,
        ds,
        es,
        ru,
        rd,
    ) = grouped(refs, (6, 4, 20, 13, 15, 14, 18, chunks, chunks, chunks, turns, turns, turns, turns))
    place = lax.axis_index("spot")
    core = lax.axis_index("gene")
    z = place // PLANE
    q = place % PLANE
    col, row = q % 2, q // 2
    mates = ((1 - row) * 2 + 1 - col, row * 2 + 1 - col, (1 - row) * 2 + col)
    others = tuple((z + step) % lines for step in range(1, lines))
    up, down = (place + PLANE, core), (place - PLANE, core)
    sibling = (place, 1 - core)
    slides, slide_rows = logits_ref.shape[0], logits_ref.shape[1]
    rows = slides * slide_rows
    cb = expr_ref.shape[0]
    genes = expr_ref.shape[1]
    last = lines - 1

    def mate(p):
        return (z * PLANE + p, core)

    def send(src, dst, send_sem, recv_sem, device):
        copy = pltpu.make_async_remote_copy(
            src_ref=src, dst_ref=dst, send_sem=send_sem, recv_sem=recv_sem, device_id=device, device_id_type=MESH
        )
        copy.start()

    def arrived(dst, recv_sem):
        pltpu.make_async_copy(dst, dst, recv_sem).wait()

    sent = arrived

    def cols(k):
        return pl.ds(sum(forward_widths[:k]), forward_widths[k])

    def turn_cols(k):
        return pl.ds(sum(backward_widths[:k]), backward_widths[k])

    def block(index):
        return pl.ds(pl.multiple_of(index * cb, cb), cb)

    def share(index):
        return pl.ds(pl.multiple_of(index * rows, rows), rows)

    def half(index):
        return pl.ds(pl.multiple_of(index * slide_rows, slide_rows), slide_rows)

    small = ((prior_in, prior_ref), (count_in, count_ref), (cells_in, cells_ref))
    pltpu.make_async_copy(expr_ref, ex, loc.at[2 * slides]).start()
    for m in range(slides):
        pltpu.make_async_copy(logits_ref.at[m], lg.at[half(m)], loc.at[m]).start()
    for at, (src, dst) in enumerate(small):
        pltpu.make_async_copy(src, dst, loc.at[2 * slides + 1 + at]).start()
    for m in range(slides):
        pltpu.make_async_copy(spatial_ref.at[m], tg.at[half(m)], loc.at[slides + m]).start()

    barrier = pltpu.get_barrier_semaphore()
    for p in mates:
        pl.semaphore_signal(barrier, inc=1, device_id=mate(p), device_id_type=MESH)
    for o in others:
        pl.semaphore_signal(barrier, inc=1, device_id=(o * PLANE + q, core), device_id_type=MESH)
    pl.semaphore_signal(barrier, inc=1, device_id=sibling, device_id_type=MESH)
    pltpu.make_async_copy(expr_ref, ex, loc.at[2 * slides]).wait()
    for k in range(chunks):
        bb[k][block(z), :] = ex[:, cols(k)]
    for m in range(slides):
        pltpu.make_async_copy(logits_ref.at[m], lg.at[half(m)], loc.at[m]).wait()
    for p in range(PLANE):
        for line in range(lines):
            lq[p, :, pl.ds(line * cb, cb)] = lg[half(core), pl.ds((line * PLANE + p) * cb, cb)]
    pl.semaphore_wait(barrier, len(mates) + len(others) + 1)

    def own_up(k):
        here = bb[k].at[block(z)]
        send(here, here, ou_s.at[k], ou_r.at[k], up)

    def own_down(k):
        here = bb[k].at[block(z)]
        send(here, here, od_s.at[k], od_r.at[k], down)

    def low(at):
        return 2 * at < lines

    for at in range(lines):

        @pl.when(z == at)
        def _():
            for k in range(chunks):
                if at < last and (at == 0 or k < (LEAD if low(at) else NEAR_LEAD)):
                    own_up(k)
                if at > 0 and (at == last or k < (NEAR_LEAD if low(at) else LEAD)):
                    own_down(k)

    for p in mates:
        send(lq.at[p], ab.at[q, half(core)], a_s, a_r.at[q], mate(p))

    def from_below(k, at):
        arrived(bb[k].at[pl.ds((at - 1) * cb, cb)], ou_r.at[k])
        if at > 1:
            arrived(bb[k].at[pl.ds(0, (at - 1) * cb)], fu_r.at[k])

    def from_above(k, at):
        arrived(bb[k].at[pl.ds((at + 1) * cb, cb)], od_r.at[k])
        if at < last - 1:
            arrived(bb[k].at[pl.ds((at + 2) * cb, (last - 1 - at) * cb)], fd_r.at[k])

    def upward(k, at):
        from_below(k, at)
        here = bb[k].at[pl.ds(0, at * cb)]
        send(here, here, fu_s.at[k], fu_r.at[k], up)

    def downward(k, at):
        from_above(k, at)
        here = bb[k].at[pl.ds((at + 1) * cb, (last - at) * cb)]
        send(here, here, fd_s.at[k], fd_r.at[k], down)

    def forward_far(k):
        for at in range(1, last):

            @pl.when(z == at)
            def _():
                (upward if low(at) else downward)(k, at)
                if k + LEAD < chunks:
                    (own_up if low(at) else own_down)(k + LEAD)

    def forward_near(k):
        for at in range(1, last):

            @pl.when(z == at)
            def _():
                (downward if low(at) else upward)(k, at)
                if k + NEAR_LEAD < chunks:
                    (own_down if low(at) else own_up)(k + NEAR_LEAD)

    def gathered(k):
        @pl.when(z == 0)
        def _():
            from_above(k, 0)

        @pl.when(z == last)
        def _():
            from_below(k, last)

    for at, (src, dst) in enumerate(small):
        pltpu.make_async_copy(src, dst, loc.at[2 * slides + 1 + at]).wait()
    weights = prior_ref[...].astype(F32) / fixed_point

    @pl.loop(0, rows // STEP_ROWS)
    def _(step):
        at = pl.ds(pl.multiple_of(step * STEP_ROWS, STEP_ROWS), STEP_ROWS)
        value = lg[at, :]
        peak = jnp.max(value, axis=1, keepdims=True)
        raised = jnp.exp(value - peak)
        scale = 1.0 / jnp.sum(raised, axis=1, keepdims=True)
        probs = raised * scale
        mass_rows = jnp.sum(probs * weights, axis=1, keepdims=True)
        rowv[0, at, :] = jnp.broadcast_to(mass_rows, (STEP_ROWS, LANES))
        rowv[1, at, :] = jnp.broadcast_to(peak, (STEP_ROWS, LANES))
        rowv[2, at, :] = jnp.broadcast_to(scale, (STEP_ROWS, LANES))
        for p in range(PLANE):
            for line in range(lines):
                at_cells = (line * PLANE + p) * cb
                pq[p, at, pl.ds(line * cb, cb)] = probs[:, at_cells : at_cells + cb]

    wide = lax.broadcasted_iota(jnp.int32, (rows, LANES), 1)
    rs[q] = jnp.where(wide == 0, rowv[1], rowv[2]).T[0:8]
    for p in mates:
        send(rs.at[q], rs.at[q], r_s, r_r.at[q], mate(p))

    rid = lax.broadcasted_iota(jnp.int32, (rows, 1), 0)
    first = rid < slide_rows
    position = place * slide_rows + jnp.where(first, rid, rid - slide_rows)
    count = jnp.where(first, count_ref[0], count_ref[1])
    valid = (position < count).astype(F32)
    scale_count = count.astype(F32)
    square = (slide_rows, slide_rows)
    eye = lax.broadcasted_iota(jnp.int32, square, 0) == lax.broadcasted_iota(jnp.int32, square, 1)
    counted = jnp.concatenate(
        [
            jnp.sum(jnp.where(eye, cells_ref[m : m + 1, :].astype(F32), 0.0), axis=1, keepdims=True)
            for m in range(slides)
        ],
        axis=0,
    )
    mass = rowv[0, :, 0:1]
    kcell = valid * counted

    def by_slide(value):
        return [jnp.sum(value[m * slide_rows : (m + 1) * slide_rows], axis=0, keepdims=True) for m in range(slides)]

    mass_parts = by_slide(valid * mass)
    cell_parts = by_slide(kcell)
    lane = lax.broadcasted_iota(jnp.int32, (1, LANES), 1)
    scalars = jnp.zeros((1, LANES), F32)
    for at, value in enumerate(mass_parts + cell_parts):
        scalars = jnp.where(lane == at, value, scalars)
    for m in range(slides):
        pltpu.make_async_copy(spatial_ref.at[m], tg.at[half(m)], loc.at[slides + m]).wait()

    head = backward_widths[0]
    t0[q] = tg[:, 0:head]
    for p in mates:
        send(t0.at[q], t0.at[q], t0_s, t0_r.at[q], mate(p))
    sacc[...] = jnp.zeros_like(sacc)
    s1[q, 3 * slides :, :] = jnp.zeros((8 - 3 * slides, genes), F32)
    s1[q, 3 * slides : 3 * slides + 1, 0:LANES] = scalars

    def share_logits():
        for p in (mates[1], mates[2], mates[0]):
            here = ab.at[p, half(core)]
            arrived(here, a_r.at[p])
            send(here, here, a2_s, a2_r.at[p], sibling)

    def lay_probs(p, at, value):
        af[p, at, :] = value
        there = pl.ds(pl.multiple_of(p * rows + at.start, BLOCK), BLOCK)
        probs_3[there, :] = threefold(value)

    def take_probs():
        in_blocks(0, rows, lambda at: lay_probs(q, at, pq[q, at, :]))
        for p in (mates[1], mates[2], mates[0]):
            arrived(rs.at[p], r_r.at[p])
            arrived(ab.at[p, half(1 - core)], a2_r.at[p])
            rowv[1] = jnp.concatenate([rs[p].T, jnp.zeros((rows, LANES - 8), F32)], axis=1)

            def take(at):
                probs = jnp.exp(ab[p, at, :] - rowv[1, at, 0:1]) * rowv[1, at, 1:2]
                lay_probs(p, at, probs)

            in_blocks(0, rows, take)

    def transpose(part):
        @pl.loop(0, PLANE // 2)
        def _(step):
            p = part * (PLANE // 2) + step
            high, low_part = halves(af[p].T)
            for third, value in enumerate((high, high, low_part)):
                turned_3[:, pl.ds(pl.multiple_of(third * PLANE * rows + p * rows, rows), rows)] = value

    def in_blocks(start, count, body):
        @pl.loop(0, count // BLOCK)
        def _(step):
            body(pl.ds(pl.multiple_of(start + step * BLOCK, BLOCK), BLOCK))

    quarter = lines * cb

    def lay_factor(at, length, width, value):
        high, low_part = halves(value)
        for third, part in enumerate((high, low_part, high)):
            here = pl.ds(pl.multiple_of(third * length + at.start, BLOCK), BLOCK)
            factor[here, 0:width] = part

    def keep_expr(k, at, value):
        start = sum(forward_widths[:k])
        for turn in range(turns):
            origin, width = sum(backward_widths[:turn]), backward_widths[turn]
            lo, hi = max(start, origin), min(start + forward_widths[k], origin + width)
            if lo < hi:
                high, low_part = halves(value[:, lo - start : hi - start])
                for third, part in enumerate((high, low_part, high)):
                    expr_3[at, pl.ds(3 * origin + third * width + lo - origin, hi - lo)] = part

    def three_turn_cols(k):
        return pl.ds(3 * sum(backward_widths[:k]), 3 * backward_widths[k])

    def forward_product(k):
        width = forward_widths[k]

        def lay(at):
            value = bb[k][at, :]
            lay_factor(at, quarter, width, value)
            keep_expr(k, at, value)

        in_blocks(0, quarter, lay)
        if k < chunks - 1:

            @pl.loop(0, PLANE * rows // TALL)
            def _(step):
                tall = pl.ds(pl.multiple_of(step * TALL, TALL), TALL)
                cs[k][tall, :] = product(probs_3[tall, :], factor[0 : 3 * quarter, 0:width], ((1,), (0,)))

            for p in mates:
                pass_pred(k, p)
        else:
            for side, served in ((1 - row, (mates[0], mates[2])), (row, (mates[1],))):
                pair = pl.ds(pl.multiple_of(2 * side * rows, 2 * rows), 2 * rows)
                cs[k][pair, :] = product(probs_3[pair, :], factor[0 : 3 * quarter, 0:width], ((1,), (0,)))
                for p in served:
                    pass_pred(k, p)

    def pass_pred(k, p):
        send(cs[k].at[share(p)], cr[k].at[q], c_s.at[k], c_r.at[k, q], mate(p))

    def finish_pred(k):
        total = cs[k][share(q), :]
        for p in mates:
            arrived(cr[k].at[p], c_r.at[k, p])
            total = total + cr[k][p]
        pr[:, cols(k)] = total
        if k == 0:
            p0[q] = total[:, 0:head]
            for p in mates:
                send(p0.at[q], p0.at[q], p0_s, p0_r.at[q], mate(p))
        truth = tg[:, cols(k)]
        for at, value in enumerate((total * truth, total * total, truth * truth)):
            sacc[at] += lane_groups(value)
        kept = valid * total
        stats = by_slide(kept * truth) + by_slide(kept * total) + by_slide(valid * truth * truth)
        s1[q, 0 : 3 * slides, cols(k)] = jnp.concatenate(stats, axis=0)

    early = sum(forward_widths[:EARLY])
    parts = (pl.ds(0, early), pl.ds(early, genes - early))

    def sum_plane(at):
        for p in mates:
            send(s1.at[q, :, parts[at]], s1.at[q, :, parts[at]], s1_s, s1_r.at[at, q], mate(p))

    def sum_line(at):
        for p in mates:
            arrived(s1.at[p, :, parts[at]], s1_r.at[at, p])
        s2[z, :, parts[at]] = (s1[0, :, parts[at]] + s1[1, :, parts[at]]) + (s1[2, :, parts[at]] + s1[3, :, parts[at]])
        for o in others:
            send(s2.at[z, :, parts[at]], s2.at[z, :, parts[at]], s2_s, s2_r.at[at, z], (o * PLANE + q, core))

    kept = {}

    def finish_genes(at):
        for o in others:
            arrived(s2.at[o, :, parts[at]], s2_r.at[at, o])
        total = s2[0, :, parts[at]]
        for line in range(1, lines):
            total = total + s2[line, :, parts[at]]
        gene_dot, gene_pred, gene_true = total[0:2], total[2:4], total[4:6]
        gene_inv = lax.rsqrt(gene_pred * gene_true + tiny)
        cos_gene = gene_dot * gene_inv
        gv[0:2, parts[at]] = gene_inv
        gv[2:4, parts[at]] = cos_gene * gene_true / (gene_pred * gene_true + tiny)
        kept["genes", at] = jnp.sum(jnp.sum(cos_gene, axis=1, keepdims=True), axis=0, keepdims=True)
        if at == 0:
            kept["mass"] = jnp.where(first, total[6:7, 0:1], total[6:7, 1:2])
            kept["cells"] = jnp.where(first, total[6:7, 2:3], total[6:7, 3:4])

    def sum_cores():
        sums = [jnp.sum(sacc[at], axis=1, keepdims=True) for at in range(3)]
        ss[core] = jnp.where(wide == 0, sums[0], jnp.where(wide == 1, sums[1], sums[2])).T[0:8]
        send(ss.at[core], ss.at[core], ss_s, ss_r, sibling)

    def finish_spots():
        lane_id = lax.broadcasted_iota(jnp.int32, (1, rows), 1)
        first_lane = lane_id < slide_rows
        lane_position = place * slide_rows + jnp.where(first_lane, lane_id, lane_id - slide_rows)
        lane_valid = (lane_position < jnp.where(first_lane, count_ref[0], count_ref[1])).astype(F32)
        arrived(ss.at[1 - core], ss_r)
        spot = ss[0] + ss[1]
        spot_dot, spot_pred, spot_true = spot[0:1], spot[1:2], spot[2:3]
        spot_inv = lax.rsqrt(spot_pred * spot_true + tiny)
        cos_spot = spot_dot * spot_inv
        spot_back = cos_spot * spot_true / (spot_pred * spot_true + tiny)
        kept["cos"] = jnp.sum(lane_valid * cos_spot, axis=1, keepdims=True)
        vectors = [lane_valid * spot_inv, lane_valid * spot_back, lane_valid, jnp.zeros((5, rows), F32)]
        vr[q] = jnp.concatenate(vectors, axis=0)
        sacc[0] = jnp.zeros_like(sacc[0])

    def gradient(truth, guess, by_row, k):
        pieces = []
        for m in range(slides):
            lo, hi = m * slide_rows, (m + 1) * slide_rows
            inverse, back = gv[m : m + 1, turn_cols(k)], gv[2 + m : 3 + m, turn_cols(k)]
            spot_inv, spot_back, spot_valid = by_row[lo:hi, 0:1], by_row[lo:hi, 1:2], by_row[lo:hi, 2:3]
            pieces.append(
                guess[lo:hi] * (spot_valid * back + spot_back) - truth[lo:hi] * (spot_valid * inverse + spot_inv)
            )
        return jnp.concatenate(pieces, axis=0)

    def head_gradient():
        for p in mates:
            arrived(t0.at[p], t0_r.at[p])
            arrived(p0.at[p], p0_r.at[p])
            arrived(vr.at[p], vr_r.at[p])
        for p in range(PLANE):
            ds[0][share(p), :] = gradient(t0[p], p0[p], vr[p].T, 0)
        sacc[0] += lane_groups(ds[0][share(q), :] * p0[q])

    def send_grad(k):
        if k == 0:
            for p in mates:
                send(vr.at[q], vr.at[q], vr_s, vr_r.at[q], mate(p))
            kept["by_row"] = vr[q].T
            return
        grad = gradient(tg[:, turn_cols(k)], pr[:, turn_cols(k)], kept["by_row"], k)
        here = ds[k].at[share(q)]
        here[...] = grad
        for p in mates:
            send(here, here, d_s.at[k], d_r.at[k, q], mate(p))
        sacc[0] += lane_groups(grad * pr[:, turn_cols(k)])

    def send_terms():
        mass_total, cell_total = kept["mass"], kept["cells"]
        portion = kcell / cell_total
        kl_rows = portion * (jnp.log(counted) - jnp.log(cell_total) - jnp.log(mass) + jnp.log(mass_total))
        dmass = scale_count * valid * (1.0 / mass_total - portion / mass)
        terms = jnp.sum(scale_count * kl_rows, axis=0, keepdims=True) - kept["cos"]
        l1[q] = jnp.broadcast_to(terms, (8, LANES))
        for p in mates:
            send(l1.at[q], l1.at[q], l1_s, l1_r.at[q], mate(p))
        inner = jnp.sum(sacc[0], axis=1, keepdims=True)
        inn[core] = jnp.where(wide == 0, inner, kept["genes", 0] + kept["genes", 1])
        send(inn.at[core], inn.at[core], in_s, in_r, sibling)
        rowv[1] = jnp.broadcast_to(dmass, (rows, LANES))

    middle = lines // 2

    def backward_product(k):
        if k == 0:
            head_gradient()
        else:
            for p in mates:
                arrived(ds[k].at[share(p)], d_r.at[k, p])
        width, spots = backward_widths[k], PLANE * rows

        def lay(at):
            value = ds[k][at, :]
            lay_factor(at, spots, width, value)
            grad_3[at, three_turn_cols(k)] = threefold(value)

        in_blocks(0, spots, lay)
        if not halved(k):

            @pl.loop(0, quarter // TALL)
            def _(step):
                tall = pl.ds(pl.multiple_of(step * TALL, TALL), TALL)
                es[k][tall, :] = product(turned_3[tall, :], factor[0 : 3 * spots, 0:width], ((1,), (0,)))

        for turn in range(2):
            if halved(k):
                side = (1 - z // middle) if turn == 0 else z // middle
                pair = pl.ds(pl.multiple_of(side * middle * cb, middle * cb), middle * cb)
                es[k][pair, :] = product(turned_3[pair, :], factor[0 : 3 * spots, 0:width], ((1,), (0,)))

            @pl.when(z == 0)
            def _():
                if halved(k):
                    pass_up(k, middle if turn == 0 else 1, middle if turn == 0 else middle - 1, turn)
                elif whole(k):
                    if turn == 0:
                        pass_up(k, 1, last, 0)
                elif turn == 0:
                    for line in range(last, 0, -1):
                        pass_up(k, line, 1, line)

            @pl.when(z == last)
            def _():
                if halved(k):
                    pass_down(k, 0 if turn == 0 else middle, middle if turn == 0 else middle - 1, turn)
                elif whole(k):
                    if turn == 0:
                        pass_down(k, 0, last, 0)
                elif turn == 0:
                    for line in range(last):
                        pass_down(k, line, 1, line)

    def halved(k):
        return k == 0

    def whole(k):
        return 0 < k < turns - SPLIT

    def pass_up(k, line, count, slot):
        here = pl.ds(line * cb, count * cb)
        send(es[k].at[here], ru[k].at[here], ru_s.at[k], ru_r.at[k, slot], up)

    def pass_down(k, line, count, slot):
        here = pl.ds(line * cb, count * cb)
        send(es[k].at[here], rd[k].at[here], rd_s.at[k], rd_r.at[k, slot], down)

    def take_up(k, line, count, slot):
        arrived(ru[k].at[pl.ds(line * cb, count * cb)], ru_r.at[k, slot])

    def take_down(k, line, count, slot):
        arrived(rd[k].at[pl.ds(line * cb, count * cb)], rd_r.at[k, slot])

    def add_up(k, line, count):
        def add(at):
            es[k][at, :] += ru[k][at, :]

        in_blocks(line * cb, count * cb, add)

    def add_down(k, line, count):
        def add(at):
            es[k][at, :] += rd[k][at, :]

        in_blocks(line * cb, count * cb, add)

    def rising(k, at):
        if halved(k) or whole(k):
            start = middle if halved(k) else at
            take_up(k, start, lines - start, 0)
            above = max(at + 1, start)
            add_up(k, above, lines - above)
            pass_up(k, above, lines - above, 0)
        else:
            for line in range(last, at, -1):
                take_up(k, line, 1, line)
                add_up(k, line, 1)
                pass_up(k, line, 1, line)

    def falling(k, at):
        if halved(k) or whole(k):
            end = middle if halved(k) else at + 1
            take_down(k, 0, end, 0)
            below = min(at, end)
            add_down(k, 0, below)
            pass_down(k, 0, below, 0)
        else:
            for line in range(at):
                take_down(k, line, 1, line)
                add_down(k, line, 1)
                pass_down(k, line, 1, line)

    def add_near(k):
        for at in range(1, last):

            @pl.when(z == at)
            def _():
                (rising if low(at) else falling)(k, at)

    def add_far(k):
        for at in range(1, last):

            @pl.when(z == at)
            def _():
                (falling if low(at) else rising)(k, at)

    def finish_expr(k):
        for at in range(lines):

            @pl.when(z == at)
            def _():
                if at > 0:
                    if halved(k) and at < middle:
                        take_up(k, at, 1, 1)
                    elif at == last and (halved(k) or whole(k)):
                        take_up(k, at, 1, 0)
                    elif not halved(k) and not whole(k):
                        take_up(k, at, 1, at)
                if at < last:
                    if halved(k) and at >= middle:
                        take_down(k, at, 1, 1)
                    elif at == 0 and (halved(k) or whole(k)):
                        take_down(k, at, 1, 0)
                    elif not halved(k) and not whole(k):
                        take_down(k, at, 1, at)

        from_low, from_high = z > 0, z < last

        @pl.loop(0, cb // BLOCK)
        def _(step):
            here = pl.ds(pl.multiple_of(step * BLOCK, BLOCK), BLOCK)
            own = pl.ds(pl.multiple_of(z * cb + step * BLOCK, BLOCK), BLOCK)
            total = es[k][own, :]
            total = total + jnp.where(from_low, ru[k][own, :], 0.0)
            ge[here, turn_cols(k)] = total + jnp.where(from_high, rd[k][own, :], 0.0)

    def probs_gradient(k):
        at = three_turn_cols(k)

        @pl.loop(0, PLANE * rows // TALL)
        def _(step):
            tall = pl.ds(pl.multiple_of(step * TALL, TALL), TALL)
            part = product(grad_3[tall, at], expr_3[:, at], ((1,), (1,)))
            if k == 0:
                fs[tall, :] = part
            else:
                fs[tall, :] += part

    def slide_of(p, m):
        return pl.ds(pl.multiple_of(p * rows + m * slide_rows, slide_rows), slide_rows)

    def sum_probs_cores():
        for p in mates + (q,):
            fx[p] = fs[slide_of(p, 1 - core), :]
            send(fx.at[p], fy.at[p], fx_s, fx_r.at[p], sibling)

    def return_probs():
        for p in mates:
            arrived(fy.at[p], fx_r.at[p])
            fz[p] = fs[slide_of(p, core), :] + fy[p]
            send(fz.at[p], fr.at[q], f_s, f_r.at[q], mate(p))
        arrived(fy.at[q], fx_r.at[q])
        fr[q] = fs[slide_of(q, core), :] + fy[q]

    def pass_terms():
        for p in mates:
            arrived(l1.at[p], l1_r.at[p])
        l2[z] = (l1[0] + l1[1]) + (l1[2] + l1[3])
        for o in others:
            send(l2.at[z], l2.at[z], l2_s, l2_r.at[z], (o * PLANE + q, core))

    def part_of(slide, m):
        start = slide * slide_rows + m * (slide_rows // 2)
        return pl.ds(pl.multiple_of(start, slide_rows // 2), slide_rows // 2)

    def finish_logits():
        arrived(inn.at[1 - core], in_r)
        rowv[2] = (inn[0] + inn[1]) + rowv[1] * rowv[0]
        for p in mates:
            arrived(fr.at[p], f_r.at[p])
        for m in range(2):

            @pl.loop(0, slide_rows // STEP_ROWS // 2)
            def _(step):
                row_at = (m * (slide_rows // STEP_ROWS // 2) + step) * STEP_ROWS
                at = pl.ds(pl.multiple_of(row_at, STEP_ROWS), STEP_ROWS)
                whole_at = pl.ds(pl.multiple_of(core * slide_rows + row_at, STEP_ROWS), STEP_ROWS)
                by_mass, total_inner = rowv[1, whole_at, 0:1], rowv[2, whole_at, 0:1]
                for p in range(PLANE):
                    for line in range(lines):
                        here, there = pl.ds(line * cb, cb), (line * PLANE + p) * cb
                        grad = fr[p, at, here] + by_mass * weights[:, there : there + cb]
                        glog[whole_at, pl.ds(there, cb)] = pq[p, whole_at, here] * (grad - total_inner)

            here = part_of(core, m)
            send(glog.at[here], glog.at[here], go_s, go_r.at[m], sibling)

    def forward_left():
        for k in range(chunks):

            @pl.when(z < last)
            def _():
                sent(bb[k].at[block(z)], ou_s.at[k])

            @pl.when(z > 0)
            def _():
                sent(bb[k].at[block(z)], od_s.at[k])

            for at in range(1, last):

                @pl.when(z == at)
                def _():
                    sent(bb[k].at[pl.ds(0, at * cb)], fu_s.at[k])
                    sent(bb[k].at[pl.ds((at + 1) * cb, (last - at) * cb)], fd_s.at[k])

        three = pl.ds(0, len(mates))
        sent(ab.at[three, half(0)], a_s)
        sent(ab.at[three, half(0)], a2_s)
        sent(rs.at[three], r_s)
        sent(t0.at[three], t0_s)
        sent(p0.at[three], p0_s)
        for k in range(chunks):
            sent(cr[k].at[three], c_s.at[k])
        sent(s1.at[three], s1_s)
        sent(s2.at[pl.ds(0, last)], s2_s)
        sent(ss.at[0], ss_s)

    steps = {
        "far": forward_far,
        "near": forward_near,
        "share": share_logits,
        "take": take_probs,
        "whole": gathered,
        "product": forward_product,
        "sum": finish_pred,
        "turn": transpose,
        "plane": sum_plane,
        "line": sum_line,
        "genes": finish_genes,
        "cores": sum_cores,
        "spots": finish_spots,
        "grad": send_grad,
        "terms": send_terms,
        "backward": backward_product,
        "probs": probs_gradient,
        "exchange": sum_probs_cores,
        "return": return_probs,
        "loss": pass_terms,
        "logits": finish_logits,
        "add_near": add_near,
        "add_far": add_far,
        "expr": finish_expr,
        "left": forward_left,
    }
    for name, *where in STEPS:
        steps[name](*where)

    for o in others:
        arrived(l2.at[o], l2_r.at[o])
    loss = l2[0]
    for line in range(1, lines):
        loss = loss + l2[line]
    loss_ref[...] = loss[0:1, 0:1] - (inn[0, 0:1, 1:2] + inn[1, 0:1, 1:2])
    for m in range(2):
        arrived(glog.at[part_of(1 - core, m)], go_r.at[m])

    for k in range(turns):
        for at in range(lines):

            @pl.when(z == at)
            def _():
                if at < last:
                    sent(es[k].at[pl.ds((at + 1) * cb, (last - at) * cb)], ru_s.at[k])
                if at > 0:
                    sent(es[k].at[pl.ds(0, at * cb)], rd_s.at[k])

    three = pl.ds(0, len(mates))
    for k in range(1, turns):
        sent(ds[k].at[pl.ds(0, len(mates) * rows)], d_s.at[k])
    sent(vr.at[three], vr_s)
    sent(inn.at[0], in_s)
    sent(l1.at[three], l1_s)
    sent(l2.at[pl.ds(0, last)], l2_s)
    sent(fr.at[three], f_s)
    sent(fx, fx_s)
    sent(glog.at[half(0)], go_s)


def lane_groups(value):
    parts = [value[:, at : at + LANES] for at in range(0, value.shape[1], LANES)]
    return functools.reduce(lambda a, b: a + b, parts)


def grouped(refs, sizes):
    at = 0
    for size in sizes:
        yield refs[at : at + size]
        at += size


def deliver(pred_in, loss_in, glog_in, gexp_in, pred_ref, loss_ref, glog_ref, gexp_ref, sems):
    slides, slide_rows = pred_ref.shape[0], pred_ref.shape[1]
    pairs = [(gexp_in, gexp_ref), (loss_in, loss_ref)]
    for m in range(slides):
        part = pl.ds(m * slide_rows, slide_rows)
        pairs += [(glog_in.at[part], glog_ref.at[m]), (pred_in.at[part], pred_ref.at[m])]
    copies = [pltpu.make_async_copy(src, dst, sems.at[at]) for at, (src, dst) in enumerate(pairs)]
    for copy in copies:
        copy.start()
    for copy in copies:
        copy.wait()


def plane_call(logits, expr, spatial, slide_spots, spot_cells, cell_prior, lines):
    slides, slide_rows, cells = logits.shape
    rows = slides * slide_rows
    cb, genes = expr.shape
    quarter = lines * cb
    spots = PLANE * rows
    chunks, turns = len(FORWARD), len(BACKWARD)
    dma = pltpu.SemaphoreType.DMA
    vmem = pltpu.VMEM
    anywhere = pl.BlockSpec(memory_space=pl.ANY)
    in_vmem = pl.BlockSpec(memory_space=pltpu.VMEM)
    scratch = [
        pltpu.SMEM((slides,), jnp.int32),
        vmem((slides, slide_rows), jnp.int32),
        vmem((1, cells), jnp.int32),
        vmem((rows, cells), F32),
        vmem((PLANE, slide_rows, quarter), F32),
        vmem((rows, genes), F32),
        vmem((cb, genes), F32),
        vmem((PLANE, rows, quarter), F32),
        vmem((PLANE, rows, quarter), F32),
        vmem((PLANE, rows, quarter), F32),
        vmem((spots, 3 * quarter), BF16),
        vmem((quarter, 3 * spots), BF16),
        vmem((quarter, 3 * genes), BF16),
        vmem((3, rows, LANES), F32),
        vmem((PLANE, 8, genes), F32),
        vmem((lines, 8, genes), F32),
        vmem((8, genes), F32),
        vmem((2, 8, rows), F32),
        vmem((3, rows, LANES), F32),
        vmem((PLANE, 8, rows), F32),
        vmem((spots, 3 * genes), BF16),
        vmem((3 * max(quarter, spots), max(FORWARD + BACKWARD)), BF16),
        vmem((PLANE, rows, BACKWARD[0]), F32),
        vmem((PLANE, rows, BACKWARD[0]), F32),
        vmem((PLANE, 8, rows), F32),
        vmem((spots, quarter), F32),
        vmem((PLANE, slide_rows, quarter), F32),
        vmem((PLANE, slide_rows, quarter), F32),
        vmem((PLANE, slide_rows, quarter), F32),
        vmem((PLANE, slide_rows, quarter), F32),
        vmem((2, rows, LANES), F32),
        vmem((PLANE, 8, LANES), F32),
        vmem((lines, 8, LANES), F32),
        dma((2 * slides + 4,)),
        dma((chunks,)),
        dma((chunks,)),
        dma((chunks,)),
        dma((chunks,)),
        dma((chunks,)),
        dma((chunks,)),
        dma((chunks,)),
        dma((chunks,)),
        dma,
        dma((PLANE,)),
        dma,
        dma((PLANE,)),
        dma,
        dma((PLANE,)),
        dma((chunks,)),
        dma((chunks, PLANE)),
        dma,
        dma((2, PLANE)),
        dma,
        dma((2, lines)),
        dma,
        dma,
        dma((turns,)),
        dma((turns, PLANE)),
        dma((turns,)),
        dma((turns, lines)),
        dma((turns,)),
        dma((turns, lines)),
        dma,
        dma((PLANE,)),
        dma,
        dma((PLANE,)),
        dma,
        dma((2,)),
        dma,
        dma,
        dma,
        dma((PLANE,)),
        dma,
        dma((lines,)),
        dma,
        dma((PLANE,)),
        dma,
        dma((PLANE,)),
        dma,
        dma((PLANE,)),
    ]
    for shape, widths in (
        ((quarter,), FORWARD),
        ((spots,), FORWARD),
        ((PLANE, rows), FORWARD),
        ((spots,), BACKWARD),
        ((quarter,), BACKWARD),
        ((quarter,), BACKWARD),
        ((quarter,), BACKWARD),
    ):
        scratch += [vmem(shape + (width,), F32) for width in widths]
    in_hbm = functools.partial(pltpu.with_memory_space_constraint, memory_space=pltpu.HBM)
    in_place = functools.partial(pltpu.with_memory_space_constraint, memory_space=pltpu.VMEM)
    results = pl.pallas_call(
        functools.partial(plane_kernel, lines, FORWARD, BACKWARD),
        out_shape=(
            vmem((rows, genes), F32),
            vmem((1, 1), F32),
            vmem((rows, cells), F32),
            vmem((cb, genes), F32),
        ),
        in_specs=[anywhere] * 6,
        out_specs=(in_vmem,) * 4,
        scratch_shapes=scratch,
        compiler_params=pltpu.CompilerParams(
            collective_id=0, has_side_effects=True, vmem_limit_bytes=48 * 1024 * 1024
        ),
    )(*map(in_hbm, (logits, expr, spatial, slide_spots, spot_cells, cell_prior.reshape(1, cells))))
    pred, loss, grad_logits, grad_expr = pl.pallas_call(
        deliver,
        out_shape=(
            jax.ShapeDtypeStruct((slides, slide_rows, genes), F32),
            jax.ShapeDtypeStruct((1, 1), F32),
            jax.ShapeDtypeStruct((slides, slide_rows, cells), F32),
            jax.ShapeDtypeStruct((cb, genes), F32),
        ),
        in_specs=[anywhere] * 4,
        out_specs=(anywhere,) * 4,
        scratch_shapes=[dma((2 * slides + 2,))],
        compiler_params=pltpu.CompilerParams(vmem_limit_bytes=4 * 1024 * 1024),
    )(*map(in_place, results))
    return pred, loss.reshape(()), grad_logits, grad_expr


def general_plan(logits, expr, spatial, slide_spots, spot_cells, cell_prior):
    place = lax.axis_index("spot")
    side = lax.axis_index("gene")
    rows_all = logits.shape[1]
    cell_rows = expr.shape[0]
    weights = cell_prior.astype(jnp.float32) / fixed_point
    gene_share = (place == 0).astype(jnp.float32)
    row_share = (side == 0).astype(jnp.float32)
    own_weights = lax.dynamic_slice_in_dim(weights, place * cell_rows, cell_rows, 0)
    expr_acc = jnp.zeros((cell_rows, expr.shape[1]), jnp.float32)
    loss_local = jnp.zeros((), jnp.float32)
    pred_list = []
    grad_list = []
    for slide in range(logits.shape[0]):
        logit_rows = logits[slide]
        counted = spot_cells[slide].astype(jnp.float32)
        target = spatial[slide]
        positions = place * rows_all + jnp.arange(rows_all, dtype=jnp.int32)
        valid = (positions < slide_spots[slide]).astype(jnp.float32)
        peak = jnp.max(logit_rows, axis=1, keepdims=True)
        raised = jnp.exp(logit_rows - peak)
        probs = raised / jnp.sum(raised, axis=1, keepdims=True)
        mass = jnp.dot(probs, weights, precision=lax.Precision.HIGHEST)
        blocks = lax.all_to_all(probs, "spot", split_axis=1, concat_axis=0, tiled=True)
        pred = lax.psum_scatter(
            jnp.dot(blocks, expr, precision=lax.Precision.HIGHEST),
            "spot",
            scatter_dimension=0,
            tiled=True,
        )
        gene_dot = jnp.sum(valid[:, None] * pred * target, axis=0)
        gene_pred = jnp.sum(valid[:, None] * pred * pred, axis=0)
        gene_true = jnp.sum(valid[:, None] * target * target, axis=0)
        mass_part = jnp.sum(valid * mass)
        kcell = valid * counted
        cell_part = jnp.sum(kcell)
        spot_dot = jnp.sum(pred * target, axis=1)
        spot_pred = jnp.sum(pred * pred, axis=1)
        spot_true = jnp.sum(target * target, axis=1)
        gene_dot, gene_pred, gene_true, mass_total, cell_total = lax.psum(
            (gene_dot, gene_pred, gene_true, mass_part, cell_part), "spot"
        )
        spot_dot, spot_pred, spot_true = lax.psum((spot_dot, spot_pred, spot_true), "gene")
        gene_inv = lax.rsqrt(gene_pred * gene_true + tiny)
        cos_gene = gene_dot * gene_inv
        spot_inv = lax.rsqrt(spot_pred * spot_true + tiny)
        cos_spot = spot_dot * spot_inv
        share = kcell / cell_total
        scale_count = slide_spots[slide].astype(jnp.float32)
        kl_part = jnp.sum(
            share * (jnp.log(counted) - jnp.log(cell_total) - jnp.log(mass) + jnp.log(mass_total))
        )
        loss_local = loss_local - gene_share * jnp.sum(cos_gene)
        loss_local = loss_local + row_share * (scale_count * kl_part - jnp.sum(valid * cos_spot))
        gene_back = cos_gene * gene_true / (gene_pred * gene_true + tiny)
        spot_back = cos_spot * spot_true / (spot_pred * spot_true + tiny)
        dpred = -valid[:, None] * (
            target * (gene_inv[None, :] + spot_inv[:, None])
            - pred * gene_back[None, :]
            - pred * spot_back[:, None]
        )
        dmass = scale_count * valid * (1.0 / mass_total - share / mass)
        pred_list.append(pred)
        grads_full, mass_full = (
            lax.all_gather(dpred, "spot", axis=0, tiled=True),
            lax.all_gather(dmass, "spot", axis=0, tiled=True),
        )
        dprob_cells = jnp.dot(grads_full, expr.T, precision=lax.Precision.HIGHEST)
        dprob_cells = lax.psum(dprob_cells, "gene")
        expr_acc = expr_acc + lax.dot_general(
            blocks, grads_full, (((0,), (0,)), ((), ())), precision=lax.Precision.HIGHEST
        )
        dprob_cells = dprob_cells + mass_full[:, None] * own_weights[None, :]
        dprob_rows = lax.all_to_all(dprob_cells, "spot", split_axis=0, concat_axis=1, tiled=True)
        inner = jnp.sum(probs * dprob_rows, axis=1, keepdims=True)
        dlogit = probs * (dprob_rows - inner)
        grad_list.append(dlogit)
    loss = lax.psum(loss_local, ("spot", "gene"))
    return (jnp.stack(pred_list), loss, jnp.stack(grad_list), expr_acc)


def solution(mesh):
    places = mesh.shape["spot"]

    def on_device(logits, expr, spatial, slide_spots, spot_cells, cell_prior):
        if places == PLANE * PLANE and mesh.shape["gene"] == 2 and expr.shape[1] == sum(FORWARD):
            return plane_call(
                logits, expr, spatial, slide_spots, spot_cells, cell_prior, places // PLANE
            )
        return general_plan(logits, expr, spatial, slide_spots, spot_cells, cell_prior)

    in_specs = (
        P(None, "spot", None),
        P("spot", "gene"),
        P(None, "spot", "gene"),
        P(),
        P(None, "spot"),
        P(),
    )
    out_specs = (P(None, "spot", "gene"), P(), P(None, "spot", None), P("spot", "gene"))
    return jax.shard_map(
        on_device, mesh=mesh, in_specs=in_specs, out_specs=out_specs, check_vma=False
    )
```

```python
import functools

import jax
import jax.numpy as jnp
from jax import lax
from jax.experimental import pallas as pl
from jax.experimental.pallas import tpu as pltpu
from jax.sharding import PartitionSpec as P

tiny = 1e-06
fixed_point = 16384.0
F32 = jnp.float32
BF16 = jnp.bfloat16
MESH = pl.DeviceIdType.MESH

PLANE = 4
LANES = 128
STEP_ROWS = 16
BLOCK = 32
TALL = 256
FORWARD = (128, 256, 256, 128, 128, 128)
BACKWARD = (128, 128, 256, 256, 256)
SPLIT = 2
LEAD = 1
NEAR_LEAD = 3
EARLY = 3
STEPS = (
    ("far", 0),
    ("far", 1),
    ("near", 0),
    ("share",),
    ("far", 2),
    ("far", 3),
    ("take",),
    ("whole", 0),
    ("near", 1),
    ("product", 0),
    ("sum", 0),
    ("whole", 1),
    ("near", 2),
    ("product", 1),
    ("whole", 2),
    ("product", 2),
    ("whole", 3),
    ("near", 3),
    ("product", 3),
    ("far", 4),
    ("whole", 4),
    ("near", 4),
    ("product", 4),
    ("sum", 1),
    ("turn", 0),
    ("far", 5),
    ("whole", 5),
    ("near", 5),
    ("product", 5),
    ("sum", 2),
    ("plane", 0),
    ("turn", 1),
    ("sum", 3),
    ("line", 0),
    ("sum", 4),
    ("sum", 5),
    ("plane", 1),
    ("cores",),
    ("genes", 0),
    ("spots",),
    ("grad", 0),
    ("grad", 1),
    ("grad", 2),
    ("line", 1),
    ("backward", 0),
    ("backward", 1),
    ("add_near", 0),
    ("genes", 1),
    ("grad", 3),
    ("backward", 2),
    ("grad", 4),
    ("probs", 0),
    ("add_far", 0),
    ("probs", 1),
    ("add_near", 1),
    ("probs", 2),
    ("terms",),
    ("backward", 3),
    ("probs", 3),
    ("add_near", 2),
    ("backward", 4),
    ("add_far", 1),
    ("probs", 4),
    ("exchange",),
    ("expr", 0),
    ("add_near", 3),
    ("add_far", 2),
    ("left",),
    ("return",),
    ("loss",),
    ("add_far", 3),
    ("expr", 1),
    ("add_near", 4),
    ("logits",),
    ("add_far", 4),
    ("expr", 2),
    ("expr", 3),
    ("expr", 4),
)


def halves(value):
    high = value.astype(BF16)
    return high, (value - high.astype(F32)).astype(BF16)


def threefold(value):
    high, low = halves(value)
    return jnp.concatenate([high, high, low], axis=1)


def product(a, b, contract):
    return lax.dot_general(a, b, (contract, ((), ())), preferred_element_type=F32)


def plane_kernel(lines, forward_widths, backward_widths, *refs):
    chunks, turns = len(forward_widths), len(backward_widths)
    (
        (logits_ref, expr_ref, spatial_ref, count_in, cells_in, prior_in),
        (pr, loss_ref, glog, ge),
        (count_ref, cells_ref, prior_ref, lg, lq, tg, ex, pq, ab, af, probs_3, turned_3, expr_3, sacc, s1, s2, gv, ss, rowv, rs),
        (grad_3, factor, t0, p0, vr, fs, fx, fy, fz, fr, inn, l1, l2),
        (loc, ou_s, ou_r, od_s, od_r, fu_s, fu_r, fd_s, fd_r, a_s, a_r, a2_s, a2_r, r_s, r_r),
        (c_s, c_r, s1_s, s1_r, s2_s, s2_r, ss_s, ss_r, d_s, d_r, ru_s, ru_r, rd_s, rd_r),
        (f_s, f_r, fx_s, fx_r, go_s, go_r, in_s, in_r, l1_s, l1_r, l2_s, l2_r, t0_s, t0_r, p0_s, p0_r, vr_s, vr_r),
        bb,
        cs,
        cr,
        ds,
        es,
        ru,
        rd,
    ) = grouped(refs, (6, 4, 20, 13, 15, 14, 18, chunks, chunks, chunks, turns, turns, turns, turns))
    place = lax.axis_index("spot")
    core = lax.axis_index("gene")
    z = place // PLANE
    q = place % PLANE
    col, row = q % 2, q // 2
    mates = ((1 - row) * 2 + 1 - col, row * 2 + 1 - col, (1 - row) * 2 + col)
    others = tuple((z + step) % lines for step in range(1, lines))
    up, down = (place + PLANE, core), (place - PLANE, core)
    sibling = (place, 1 - core)
    slides, slide_rows = logits_ref.shape[0], logits_ref.shape[1]
    rows = slides * slide_rows
    cb = expr_ref.shape[0]
    genes = expr_ref.shape[1]
    last = lines - 1

    def mate(p):
        return (z * PLANE + p, core)

    def send(src, dst, send_sem, recv_sem, device):
        copy = pltpu.make_async_remote_copy(
            src_ref=src, dst_ref=dst, send_sem=send_sem, recv_sem=recv_sem, device_id=device, device_id_type=MESH
        )
        copy.start()

    def arrived(dst, recv_sem):
        pltpu.make_async_copy(dst, dst, recv_sem).wait()

    sent = arrived

    def cols(k):
        return pl.ds(sum(forward_widths[:k]), forward_widths[k])

    def turn_cols(k):
        return pl.ds(sum(backward_widths[:k]), backward_widths[k])

    def block(index):
        return pl.ds(pl.multiple_of(index * cb, cb), cb)

    def share(index):
        return pl.ds(pl.multiple_of(index * rows, rows), rows)

    def half(index):
        return pl.ds(pl.multiple_of(index * slide_rows, slide_rows), slide_rows)

    small = ((prior_in, prior_ref), (count_in, count_ref), (cells_in, cells_ref))
    pltpu.make_async_copy(expr_ref, ex, loc.at[2 * slides]).start()
    for m in range(slides):
        pltpu.make_async_copy(logits_ref.at[m], lg.at[half(m)], loc.at[m]).start()
    for at, (src, dst) in enumerate(small):
        pltpu.make_async_copy(src, dst, loc.at[2 * slides + 1 + at]).start()
    for m in range(slides):
        pltpu.make_async_copy(spatial_ref.at[m], tg.at[half(m)], loc.at[slides + m]).start()

    barrier = pltpu.get_barrier_semaphore()
    for p in mates:
        pl.semaphore_signal(barrier, inc=1, device_id=mate(p), device_id_type=MESH)
    for o in others:
        pl.semaphore_signal(barrier, inc=1, device_id=(o * PLANE + q, core), device_id_type=MESH)
    pl.semaphore_signal(barrier, inc=1, device_id=sibling, device_id_type=MESH)
    pltpu.make_async_copy(expr_ref, ex, loc.at[2 * slides]).wait()
    for k in range(chunks):
        bb[k][block(z), :] = ex[:, cols(k)]
    for m in range(slides):
        pltpu.make_async_copy(logits_ref.at[m], lg.at[half(m)], loc.at[m]).wait()
    for p in range(PLANE):
        for line in range(lines):
            lq[p, :, pl.ds(line * cb, cb)] = lg[half(core), pl.ds((line * PLANE + p) * cb, cb)]
    pl.semaphore_wait(barrier, len(mates) + len(others) + 1)

    def own_up(k):
        here = bb[k].at[block(z)]
        send(here, here, ou_s.at[k], ou_r.at[k], up)

    def own_down(k):
        here = bb[k].at[block(z)]
        send(here, here, od_s.at[k], od_r.at[k], down)

    def low(at):
        return 2 * at < lines

    for at in range(lines):

        @pl.when(z == at)
        def _():
            for k in range(chunks):
                if at < last and (at == 0 or k < (LEAD if low(at) else NEAR_LEAD)):
                    own_up(k)
                if at > 0 and (at == last or k < (NEAR_LEAD if low(at) else LEAD)):
                    own_down(k)

    for p in mates:
        send(lq.at[p], ab.at[q, half(core)], a_s, a_r.at[q], mate(p))

    def from_below(k, at):
        arrived(bb[k].at[pl.ds((at - 1) * cb, cb)], ou_r.at[k])
        if at > 1:
            arrived(bb[k].at[pl.ds(0, (at - 1) * cb)], fu_r.at[k])

    def from_above(k, at):
        arrived(bb[k].at[pl.ds((at + 1) * cb, cb)], od_r.at[k])
        if at < last - 1:
            arrived(bb[k].at[pl.ds((at + 2) * cb, (last - 1 - at) * cb)], fd_r.at[k])

    def upward(k, at):
        from_below(k, at)
        here = bb[k].at[pl.ds(0, at * cb)]
        send(here, here, fu_s.at[k], fu_r.at[k], up)

    def downward(k, at):
        from_above(k, at)
        here = bb[k].at[pl.ds((at + 1) * cb, (last - at) * cb)]
        send(here, here, fd_s.at[k], fd_r.at[k], down)

    def forward_far(k):
        for at in range(1, last):

            @pl.when(z == at)
            def _():
                (upward if low(at) else downward)(k, at)
                if k + LEAD < chunks:
                    (own_up if low(at) else own_down)(k + LEAD)

    def forward_near(k):
        for at in range(1, last):

            @pl.when(z == at)
            def _():
                (downward if low(at) else upward)(k, at)
                if k + NEAR_LEAD < chunks:
                    (own_down if low(at) else own_up)(k + NEAR_LEAD)

    def gathered(k):
        @pl.when(z == 0)
        def _():
            from_above(k, 0)

        @pl.when(z == last)
        def _():
            from_below(k, last)

    for at, (src, dst) in enumerate(small):
        pltpu.make_async_copy(src, dst, loc.at[2 * slides + 1 + at]).wait()
    weights = prior_ref[...].astype(F32) / fixed_point

    @pl.loop(0, rows // STEP_ROWS)
    def _(step):
        at = pl.ds(pl.multiple_of(step * STEP_ROWS, STEP_ROWS), STEP_ROWS)
        value = lg[at, :]
        peak = jnp.max(value, axis=1, keepdims=True)
        raised = jnp.exp(value - peak)
        scale = 1.0 / jnp.sum(raised, axis=1, keepdims=True)
        probs = raised * scale
        mass_rows = jnp.sum(probs * weights, axis=1, keepdims=True)
        rowv[0, at, :] = jnp.broadcast_to(mass_rows, (STEP_ROWS, LANES))
        rowv[1, at, :] = jnp.broadcast_to(peak, (STEP_ROWS, LANES))
        rowv[2, at, :] = jnp.broadcast_to(scale, (STEP_ROWS, LANES))
        for p in range(PLANE):
            for line in range(lines):
                at_cells = (line * PLANE + p) * cb
                pq[p, at, pl.ds(line * cb, cb)] = probs[:, at_cells : at_cells + cb]

    wide = lax.broadcasted_iota(jnp.int32, (rows, LANES), 1)
    rs[q] = jnp.where(wide == 0, rowv[1], rowv[2]).T[0:8]
    for p in mates:
        send(rs.at[q], rs.at[q], r_s, r_r.at[q], mate(p))

    rid = lax.broadcasted_iota(jnp.int32, (rows, 1), 0)
    first = rid < slide_rows
    position = place * slide_rows + jnp.where(first, rid, rid - slide_rows)
    count = jnp.where(first, count_ref[0], count_ref[1])
    valid = (position < count).astype(F32)
    scale_count = count.astype(F32)
    square = (slide_rows, slide_rows)
    eye = lax.broadcasted_iota(jnp.int32, square, 0) == lax.broadcasted_iota(jnp.int32, square, 1)
    counted = jnp.concatenate(
        [
            jnp.sum(jnp.where(eye, cells_ref[m : m + 1, :].astype(F32), 0.0), axis=1, keepdims=True)
            for m in range(slides)
        ],
        axis=0,
    )
    mass = rowv[0, :, 0:1]
    kcell = valid * counted

    def by_slide(value):
        return [jnp.sum(value[m * slide_rows : (m + 1) * slide_rows], axis=0, keepdims=True) for m in range(slides)]

    mass_parts = by_slide(valid * mass)
    cell_parts = by_slide(kcell)
    lane = lax.broadcasted_iota(jnp.int32, (1, LANES), 1)
    scalars = jnp.zeros((1, LANES), F32)
    for at, value in enumerate(mass_parts + cell_parts):
        scalars = jnp.where(lane == at, value, scalars)
    for m in range(slides):
        pltpu.make_async_copy(spatial_ref.at[m], tg.at[half(m)], loc.at[slides + m]).wait()

    head = backward_widths[0]
    t0[q] = tg[:, 0:head]
    for p in mates:
        send(t0.at[q], t0.at[q], t0_s, t0_r.at[q], mate(p))
    sacc[...] = jnp.zeros_like(sacc)
    s1[q, 3 * slides :, :] = jnp.zeros((8 - 3 * slides, genes), F32)
    s1[q, 3 * slides : 3 * slides + 1, 0:LANES] = scalars

    def share_logits():
        for p in (mates[1], mates[2], mates[0]):
            here = ab.at[p, half(core)]
            arrived(here, a_r.at[p])
            send(here, here, a2_s, a2_r.at[p], sibling)

    def lay_probs(p, at, value):
        af[p, at, :] = value
        there = pl.ds(pl.multiple_of(p * rows + at.start, BLOCK), BLOCK)
        probs_3[there, :] = threefold(value)

    def take_probs():
        in_blocks(0, rows, lambda at: lay_probs(q, at, pq[q, at, :]))
        for p in (mates[1], mates[2], mates[0]):
            arrived(rs.at[p], r_r.at[p])
            arrived(ab.at[p, half(1 - core)], a2_r.at[p])
            rowv[1] = jnp.concatenate([rs[p].T, jnp.zeros((rows, LANES - 8), F32)], axis=1)

            def take(at):
                probs = jnp.exp(ab[p, at, :] - rowv[1, at, 0:1]) * rowv[1, at, 1:2]
                lay_probs(p, at, probs)

            in_blocks(0, rows, take)

    def transpose(part):
        @pl.loop(0, PLANE // 2)
        def _(step):
            p = part * (PLANE // 2) + step
            high, low_part = halves(af[p].T)
            for third, value in enumerate((high, high, low_part)):
                turned_3[:, pl.ds(pl.multiple_of(third * PLANE * rows + p * rows, rows), rows)] = value

    def in_blocks(start, count, body):
        @pl.loop(0, count // BLOCK)
        def _(step):
            body(pl.ds(pl.multiple_of(start + step * BLOCK, BLOCK), BLOCK))

    quarter = lines * cb

    def lay_factor(at, length, width, value):
        high, low_part = halves(value)
        for third, part in enumerate((high, low_part, high)):
            here = pl.ds(pl.multiple_of(third * length + at.start, BLOCK), BLOCK)
            factor[here, 0:width] = part

    def keep_expr(k, at, value):
        start = sum(forward_widths[:k])
        for turn in range(turns):
            origin, width = sum(backward_widths[:turn]), backward_widths[turn]
            lo, hi = max(start, origin), min(start + forward_widths[k], origin + width)
            if lo < hi:
                high, low_part = halves(value[:, lo - start : hi - start])
                for third, part in enumerate((high, low_part, high)):
                    expr_3[at, pl.ds(3 * origin + third * width + lo - origin, hi - lo)] = part

    def three_turn_cols(k):
        return pl.ds(3 * sum(backward_widths[:k]), 3 * backward_widths[k])

    def forward_product(k):
        width = forward_widths[k]

        def lay(at):
            value = bb[k][at, :]
            lay_factor(at, quarter, width, value)
            keep_expr(k, at, value)

        in_blocks(0, quarter, lay)
        if k < chunks - 1:

            @pl.loop(0, PLANE * rows // TALL)
            def _(step):
                tall = pl.ds(pl.multiple_of(step * TALL, TALL), TALL)
                cs[k][tall, :] = product(probs_3[tall, :], factor[0 : 3 * quarter, 0:width], ((1,), (0,)))

            for p in mates:
                pass_pred(k, p)
        else:
            for side, served in ((1 - row, (mates[0], mates[2])), (row, (mates[1],))):
                pair = pl.ds(pl.multiple_of(2 * side * rows, 2 * rows), 2 * rows)
                cs[k][pair, :] = product(probs_3[pair, :], factor[0 : 3 * quarter, 0:width], ((1,), (0,)))
                for p in served:
                    pass_pred(k, p)

    def pass_pred(k, p):
        send(cs[k].at[share(p)], cr[k].at[q], c_s.at[k], c_r.at[k, q], mate(p))

    def finish_pred(k):
        total = cs[k][share(q), :]
        for p in mates:
            arrived(cr[k].at[p], c_r.at[k, p])
            total = total + cr[k][p]
        pr[:, cols(k)] = total
        if k == 0:
            p0[q] = total[:, 0:head]
            for p in mates:
                send(p0.at[q], p0.at[q], p0_s, p0_r.at[q], mate(p))
        truth = tg[:, cols(k)]
        for at, value in enumerate((total * truth, total * total, truth * truth)):
            sacc[at] += lane_groups(value)
        kept = valid * total
        stats = by_slide(kept * truth) + by_slide(kept * total) + by_slide(valid * truth * truth)
        s1[q, 0 : 3 * slides, cols(k)] = jnp.concatenate(stats, axis=0)

    early = sum(forward_widths[:EARLY])
    parts = (pl.ds(0, early), pl.ds(early, genes - early))

    def sum_plane(at):
        for p in mates:
            send(s1.at[q, :, parts[at]], s1.at[q, :, parts[at]], s1_s, s1_r.at[at, q], mate(p))

    def sum_line(at):
        for p in mates:
            arrived(s1.at[p, :, parts[at]], s1_r.at[at, p])
        s2[z, :, parts[at]] = (s1[0, :, parts[at]] + s1[1, :, parts[at]]) + (s1[2, :, parts[at]] + s1[3, :, parts[at]])
        for o in others:
            send(s2.at[z, :, parts[at]], s2.at[z, :, parts[at]], s2_s, s2_r.at[at, z], (o * PLANE + q, core))

    kept = {}

    def finish_genes(at):
        for o in others:
            arrived(s2.at[o, :, parts[at]], s2_r.at[at, o])
        total = s2[0, :, parts[at]]
        for line in range(1, lines):
            total = total + s2[line, :, parts[at]]
        gene_dot, gene_pred, gene_true = total[0:2], total[2:4], total[4:6]
        gene_inv = lax.rsqrt(gene_pred * gene_true + tiny)
        cos_gene = gene_dot * gene_inv
        gv[0:2, parts[at]] = gene_inv
        gv[2:4, parts[at]] = cos_gene * gene_true / (gene_pred * gene_true + tiny)
        kept["genes", at] = jnp.sum(jnp.sum(cos_gene, axis=1, keepdims=True), axis=0, keepdims=True)
        if at == 0:
            kept["mass"] = jnp.where(first, total[6:7, 0:1], total[6:7, 1:2])
            kept["cells"] = jnp.where(first, total[6:7, 2:3], total[6:7, 3:4])

    def sum_cores():
        sums = [jnp.sum(sacc[at], axis=1, keepdims=True) for at in range(3)]
        ss[core] = jnp.where(wide == 0, sums[0], jnp.where(wide == 1, sums[1], sums[2])).T[0:8]
        send(ss.at[core], ss.at[core], ss_s, ss_r, sibling)

    def finish_spots():
        lane_id = lax.broadcasted_iota(jnp.int32, (1, rows), 1)
        first_lane = lane_id < slide_rows
        lane_position = place * slide_rows + jnp.where(first_lane, lane_id, lane_id - slide_rows)
        lane_valid = (lane_position < jnp.where(first_lane, count_ref[0], count_ref[1])).astype(F32)
        arrived(ss.at[1 - core], ss_r)
        spot = ss[0] + ss[1]
        spot_dot, spot_pred, spot_true = spot[0:1], spot[1:2], spot[2:3]
        spot_inv = lax.rsqrt(spot_pred * spot_true + tiny)
        cos_spot = spot_dot * spot_inv
        spot_back = cos_spot * spot_true / (spot_pred * spot_true + tiny)
        kept["cos"] = jnp.sum(lane_valid * cos_spot, axis=1, keepdims=True)
        vectors = [lane_valid * spot_inv, lane_valid * spot_back, lane_valid, jnp.zeros((5, rows), F32)]
        vr[q] = jnp.concatenate(vectors, axis=0)
        sacc[0] = jnp.zeros_like(sacc[0])

    def gradient(truth, guess, by_row, k):
        pieces = []
        for m in range(slides):
            lo, hi = m * slide_rows, (m + 1) * slide_rows
            inverse, back = gv[m : m + 1, turn_cols(k)], gv[2 + m : 3 + m, turn_cols(k)]
            spot_inv, spot_back, spot_valid = by_row[lo:hi, 0:1], by_row[lo:hi, 1:2], by_row[lo:hi, 2:3]
            pieces.append(
                guess[lo:hi] * (spot_valid * back + spot_back) - truth[lo:hi] * (spot_valid * inverse + spot_inv)
            )
        return jnp.concatenate(pieces, axis=0)

    def head_gradient():
        for p in mates:
            arrived(t0.at[p], t0_r.at[p])
            arrived(p0.at[p], p0_r.at[p])
            arrived(vr.at[p], vr_r.at[p])
        for p in range(PLANE):
            ds[0][share(p), :] = gradient(t0[p], p0[p], vr[p].T, 0)
        sacc[0] += lane_groups(ds[0][share(q), :] * p0[q])

    def send_grad(k):
        if k == 0:
            for p in mates:
                send(vr.at[q], vr.at[q], vr_s, vr_r.at[q], mate(p))
            kept["by_row"] = vr[q].T
            return
        grad = gradient(tg[:, turn_cols(k)], pr[:, turn_cols(k)], kept["by_row"], k)
        here = ds[k].at[share(q)]
        here[...] = grad
        for p in mates:
            send(here, here, d_s.at[k], d_r.at[k, q], mate(p))
        sacc[0] += lane_groups(grad * pr[:, turn_cols(k)])

    def send_terms():
        mass_total, cell_total = kept["mass"], kept["cells"]
        portion = kcell / cell_total
        kl_rows = portion * (jnp.log(counted) - jnp.log(cell_total) - jnp.log(mass) + jnp.log(mass_total))
        dmass = scale_count * valid * (1.0 / mass_total - portion / mass)
        terms = jnp.sum(scale_count * kl_rows, axis=0, keepdims=True) - kept["cos"]
        l1[q] = jnp.broadcast_to(terms, (8, LANES))
        for p in mates:
            send(l1.at[q], l1.at[q], l1_s, l1_r.at[q], mate(p))
        inner = jnp.sum(sacc[0], axis=1, keepdims=True)
        inn[core] = jnp.where(wide == 0, inner, kept["genes", 0] + kept["genes", 1])
        send(inn.at[core], inn.at[core], in_s, in_r, sibling)
        rowv[1] = jnp.broadcast_to(dmass, (rows, LANES))

    middle = lines // 2

    def backward_product(k):
        if k == 0:
            head_gradient()
        else:
            for p in mates:
                arrived(ds[k].at[share(p)], d_r.at[k, p])
        width, spots = backward_widths[k], PLANE * rows

        def lay(at):
            value = ds[k][at, :]
            lay_factor(at, spots, width, value)
            grad_3[at, three_turn_cols(k)] = threefold(value)

        in_blocks(0, spots, lay)
        if not halved(k):

            @pl.loop(0, quarter // TALL)
            def _(step):
                tall = pl.ds(pl.multiple_of(step * TALL, TALL), TALL)
                es[k][tall, :] = product(turned_3[tall, :], factor[0 : 3 * spots, 0:width], ((1,), (0,)))

        for turn in range(2):
            if halved(k):
                side = (1 - z // middle) if turn == 0 else z // middle
                pair = pl.ds(pl.multiple_of(side * middle * cb, middle * cb), middle * cb)
                es[k][pair, :] = product(turned_3[pair, :], factor[0 : 3 * spots, 0:width], ((1,), (0,)))

            @pl.when(z == 0)
            def _():
                if halved(k):
                    pass_up(k, middle if turn == 0 else 1, middle if turn == 0 else middle - 1, turn)
                elif whole(k):
                    if turn == 0:
                        pass_up(k, 1, last, 0)
                elif turn == 0:
                    for line in range(last, 0, -1):
                        pass_up(k, line, 1, line)

            @pl.when(z == last)
            def _():
                if halved(k):
                    pass_down(k, 0 if turn == 0 else middle, middle if turn == 0 else middle - 1, turn)
                elif whole(k):
                    if turn == 0:
                        pass_down(k, 0, last, 0)
                elif turn == 0:
                    for line in range(last):
                        pass_down(k, line, 1, line)

    def halved(k):
        return k == 0

    def whole(k):
        return 0 < k < turns - SPLIT

    def pass_up(k, line, count, slot):
        here = pl.ds(line * cb, count * cb)
        send(es[k].at[here], ru[k].at[here], ru_s.at[k], ru_r.at[k, slot], up)

    def pass_down(k, line, count, slot):
        here = pl.ds(line * cb, count * cb)
        send(es[k].at[here], rd[k].at[here], rd_s.at[k], rd_r.at[k, slot], down)

    def take_up(k, line, count, slot):
        arrived(ru[k].at[pl.ds(line * cb, count * cb)], ru_r.at[k, slot])

    def take_down(k, line, count, slot):
        arrived(rd[k].at[pl.ds(line * cb, count * cb)], rd_r.at[k, slot])

    def add_up(k, line, count):
        def add(at):
            es[k][at, :] += ru[k][at, :]

        in_blocks(line * cb, count * cb, add)

    def add_down(k, line, count):
        def add(at):
            es[k][at, :] += rd[k][at, :]

        in_blocks(line * cb, count * cb, add)

    def rising(k, at):
        if halved(k) or whole(k):
            start = middle if halved(k) else at
            take_up(k, start, lines - start, 0)
            above = max(at + 1, start)
            add_up(k, above, lines - above)
            pass_up(k, above, lines - above, 0)
        else:
            for line in range(last, at, -1):
                take_up(k, line, 1, line)
                add_up(k, line, 1)
                pass_up(k, line, 1, line)

    def falling(k, at):
        if halved(k) or whole(k):
            end = middle if halved(k) else at + 1
            take_down(k, 0, end, 0)
            below = min(at, end)
            add_down(k, 0, below)
            pass_down(k, 0, below, 0)
        else:
            for line in range(at):
                take_down(k, line, 1, line)
                add_down(k, line, 1)
                pass_down(k, line, 1, line)

    def add_near(k):
        for at in range(1, last):

            @pl.when(z == at)
            def _():
                (rising if low(at) else falling)(k, at)

    def add_far(k):
        for at in range(1, last):

            @pl.when(z == at)
            def _():
                (falling if low(at) else rising)(k, at)

    def finish_expr(k):
        for at in range(lines):

            @pl.when(z == at)
            def _():
                if at > 0:
                    if halved(k) and at < middle:
                        take_up(k, at, 1, 1)
                    elif at == last and (halved(k) or whole(k)):
                        take_up(k, at, 1, 0)
                    elif not halved(k) and not whole(k):
                        take_up(k, at, 1, at)
                if at < last:
                    if halved(k) and at >= middle:
                        take_down(k, at, 1, 1)
                    elif at == 0 and (halved(k) or whole(k)):
                        take_down(k, at, 1, 0)
                    elif not halved(k) and not whole(k):
                        take_down(k, at, 1, at)

        from_low, from_high = z > 0, z < last

        @pl.loop(0, cb // BLOCK)
        def _(step):
            here = pl.ds(pl.multiple_of(step * BLOCK, BLOCK), BLOCK)
            own = pl.ds(pl.multiple_of(z * cb + step * BLOCK, BLOCK), BLOCK)
            total = es[k][own, :]
            total = total + jnp.where(from_low, ru[k][own, :], 0.0)
            ge[here, turn_cols(k)] = total + jnp.where(from_high, rd[k][own, :], 0.0)

    def probs_gradient(k):
        at = three_turn_cols(k)

        @pl.loop(0, PLANE * rows // TALL)
        def _(step):
            tall = pl.ds(pl.multiple_of(step * TALL, TALL), TALL)
            part = product(grad_3[tall, at], expr_3[:, at], ((1,), (1,)))
            if k == 0:
                fs[tall, :] = part
            else:
                fs[tall, :] += part

    def slide_of(p, m):
        return pl.ds(pl.multiple_of(p * rows + m * slide_rows, slide_rows), slide_rows)

    def sum_probs_cores():
        for p in mates + (q,):
            fx[p] = fs[slide_of(p, 1 - core), :]
            send(fx.at[p], fy.at[p], fx_s, fx_r.at[p], sibling)

    def return_probs():
        for p in mates:
            arrived(fy.at[p], fx_r.at[p])
            fz[p] = fs[slide_of(p, core), :] + fy[p]
            send(fz.at[p], fr.at[q], f_s, f_r.at[q], mate(p))
        arrived(fy.at[q], fx_r.at[q])
        fr[q] = fs[slide_of(q, core), :] + fy[q]

    def pass_terms():
        for p in mates:
            arrived(l1.at[p], l1_r.at[p])
        l2[z] = (l1[0] + l1[1]) + (l1[2] + l1[3])
        for o in others:
            send(l2.at[z], l2.at[z], l2_s, l2_r.at[z], (o * PLANE + q, core))

    def part_of(slide, m):
        start = slide * slide_rows + m * (slide_rows // 2)
        return pl.ds(pl.multiple_of(start, slide_rows // 2), slide_rows // 2)

    def finish_logits():
        arrived(inn.at[1 - core], in_r)
        rowv[2] = (inn[0] + inn[1]) + rowv[1] * rowv[0]
        for p in mates:
            arrived(fr.at[p], f_r.at[p])
        for m in range(2):

            @pl.loop(0, slide_rows // STEP_ROWS // 2)
            def _(step):
                row_at = (m * (slide_rows // STEP_ROWS // 2) + step) * STEP_ROWS
                at = pl.ds(pl.multiple_of(row_at, STEP_ROWS), STEP_ROWS)
                whole_at = pl.ds(pl.multiple_of(core * slide_rows + row_at, STEP_ROWS), STEP_ROWS)
                by_mass, total_inner = rowv[1, whole_at, 0:1], rowv[2, whole_at, 0:1]
                for p in range(PLANE):
                    for line in range(lines):
                        here, there = pl.ds(line * cb, cb), (line * PLANE + p) * cb
                        grad = fr[p, at, here] + by_mass * weights[:, there : there + cb]
                        glog[whole_at, pl.ds(there, cb)] = pq[p, whole_at, here] * (grad - total_inner)

            here = part_of(core, m)
            send(glog.at[here], glog.at[here], go_s, go_r.at[m], sibling)

    def forward_left():
        for k in range(chunks):

            @pl.when(z < last)
            def _():
                sent(bb[k].at[block(z)], ou_s.at[k])

            @pl.when(z > 0)
            def _():
                sent(bb[k].at[block(z)], od_s.at[k])

            for at in range(1, last):

                @pl.when(z == at)
                def _():
                    sent(bb[k].at[pl.ds(0, at * cb)], fu_s.at[k])
                    sent(bb[k].at[pl.ds((at + 1) * cb, (last - at) * cb)], fd_s.at[k])

        three = pl.ds(0, len(mates))
        sent(ab.at[three, half(0)], a_s)
        sent(ab.at[three, half(0)], a2_s)
        sent(rs.at[three], r_s)
        sent(t0.at[three], t0_s)
        sent(p0.at[three], p0_s)
        for k in range(chunks):
            sent(cr[k].at[three], c_s.at[k])
        sent(s1.at[three], s1_s)
        sent(s2.at[pl.ds(0, last)], s2_s)
        sent(ss.at[0], ss_s)

    steps = {
        "far": forward_far,
        "near": forward_near,
        "share": share_logits,
        "take": take_probs,
        "whole": gathered,
        "product": forward_product,
        "sum": finish_pred,
        "turn": transpose,
        "plane": sum_plane,
        "line": sum_line,
        "genes": finish_genes,
        "cores": sum_cores,
        "spots": finish_spots,
        "grad": send_grad,
        "terms": send_terms,
        "backward": backward_product,
        "probs": probs_gradient,
        "exchange": sum_probs_cores,
        "return": return_probs,
        "loss": pass_terms,
        "logits": finish_logits,
        "add_near": add_near,
        "add_far": add_far,
        "expr": finish_expr,
        "left": forward_left,
    }
    for name, *where in STEPS:
        steps[name](*where)

    for o in others:
        arrived(l2.at[o], l2_r.at[o])
    loss = l2[0]
    for line in range(1, lines):
        loss = loss + l2[line]
    loss_ref[...] = loss[0:1, 0:1] - (inn[0, 0:1, 1:2] + inn[1, 0:1, 1:2])
    for m in range(2):
        arrived(glog.at[part_of(1 - core, m)], go_r.at[m])

    for k in range(turns):
        for at in range(lines):

            @pl.when(z == at)
            def _():
                if at < last:
                    sent(es[k].at[pl.ds((at + 1) * cb, (last - at) * cb)], ru_s.at[k])
                if at > 0:
                    sent(es[k].at[pl.ds(0, at * cb)], rd_s.at[k])

    three = pl.ds(0, len(mates))
    for k in range(1, turns):
        sent(ds[k].at[pl.ds(0, len(mates) * rows)], d_s.at[k])
    sent(vr.at[three], vr_s)
    sent(inn.at[0], in_s)
    sent(l1.at[three], l1_s)
    sent(l2.at[pl.ds(0, last)], l2_s)
    sent(fr.at[three], f_s)
    sent(fx, fx_s)
    sent(glog.at[half(0)], go_s)


def lane_groups(value):
    parts = [value[:, at : at + LANES] for at in range(0, value.shape[1], LANES)]
    return functools.reduce(lambda a, b: a + b, parts)


def grouped(refs, sizes):
    at = 0
    for size in sizes:
        yield refs[at : at + size]
        at += size


def deliver(pred_in, loss_in, glog_in, gexp_in, pred_ref, loss_ref, glog_ref, gexp_ref, sems):
    slides, slide_rows = pred_ref.shape[0], pred_ref.shape[1]
    pairs = [(gexp_in, gexp_ref), (loss_in, loss_ref)]
    for m in range(slides):
        part = pl.ds(m * slide_rows, slide_rows)
        pairs += [(glog_in.at[part], glog_ref.at[m]), (pred_in.at[part], pred_ref.at[m])]
    copies = [pltpu.make_async_copy(src, dst, sems.at[at]) for at, (src, dst) in enumerate(pairs)]
    for copy in copies:
        copy.start()
    for copy in copies:
        copy.wait()


def plane_call(logits, expr, spatial, slide_spots, spot_cells, cell_prior, lines):
    slides, slide_rows, cells = logits.shape
    rows = slides * slide_rows
    cb, genes = expr.shape
    quarter = lines * cb
    spots = PLANE * rows
    chunks, turns = len(FORWARD), len(BACKWARD)
    dma = pltpu.SemaphoreType.DMA
    vmem = pltpu.VMEM
    anywhere = pl.BlockSpec(memory_space=pl.ANY)
    in_vmem = pl.BlockSpec(memory_space=pltpu.VMEM)
    scratch = [
        pltpu.SMEM((slides,), jnp.int32),
        vmem((slides, slide_rows), jnp.int32),
        vmem((1, cells), jnp.int32),
        vmem((rows, cells), F32),
        vmem((PLANE, slide_rows, quarter), F32),
        vmem((rows, genes), F32),
        vmem((cb, genes), F32),
        vmem((PLANE, rows, quarter), F32),
        vmem((PLANE, rows, quarter), F32),
        vmem((PLANE, rows, quarter), F32),
        vmem((spots, 3 * quarter), BF16),
        vmem((quarter, 3 * spots), BF16),
        vmem((quarter, 3 * genes), BF16),
        vmem((3, rows, LANES), F32),
        vmem((PLANE, 8, genes), F32),
        vmem((lines, 8, genes), F32),
        vmem((8, genes), F32),
        vmem((2, 8, rows), F32),
        vmem((3, rows, LANES), F32),
        vmem((PLANE, 8, rows), F32),
        vmem((spots, 3 * genes), BF16),
        vmem((3 * max(quarter, spots), max(FORWARD + BACKWARD)), BF16),
        vmem((PLANE, rows, BACKWARD[0]), F32),
        vmem((PLANE, rows, BACKWARD[0]), F32),
        vmem((PLANE, 8, rows), F32),
        vmem((spots, quarter), F32),
        vmem((PLANE, slide_rows, quarter), F32),
        vmem((PLANE, slide_rows, quarter), F32),
        vmem((PLANE, slide_rows, quarter), F32),
        vmem((PLANE, slide_rows, quarter), F32),
        vmem((2, rows, LANES), F32),
        vmem((PLANE, 8, LANES), F32),
        vmem((lines, 8, LANES), F32),
        dma((2 * slides + 4,)),
        dma((chunks,)),
        dma((chunks,)),
        dma((chunks,)),
        dma((chunks,)),
        dma((chunks,)),
        dma((chunks,)),
        dma((chunks,)),
        dma((chunks,)),
        dma,
        dma((PLANE,)),
        dma,
        dma((PLANE,)),
        dma,
        dma((PLANE,)),
        dma((chunks,)),
        dma((chunks, PLANE)),
        dma,
        dma((2, PLANE)),
        dma,
        dma((2, lines)),
        dma,
        dma,
        dma((turns,)),
        dma((turns, PLANE)),
        dma((turns,)),
        dma((turns, lines)),
        dma((turns,)),
        dma((turns, lines)),
        dma,
        dma((PLANE,)),
        dma,
        dma((PLANE,)),
        dma,
        dma((2,)),
        dma,
        dma,
        dma,
        dma((PLANE,)),
        dma,
        dma((lines,)),
        dma,
        dma((PLANE,)),
        dma,
        dma((PLANE,)),
        dma,
        dma((PLANE,)),
    ]
    for shape, widths in (
        ((quarter,), FORWARD),
        ((spots,), FORWARD),
        ((PLANE, rows), FORWARD),
        ((spots,), BACKWARD),
        ((quarter,), BACKWARD),
        ((quarter,), BACKWARD),
        ((quarter,), BACKWARD),
    ):
        scratch += [vmem(shape + (width,), F32) for width in widths]
    in_hbm = functools.partial(pltpu.with_memory_space_constraint, memory_space=pltpu.HBM)
    in_place = functools.partial(pltpu.with_memory_space_constraint, memory_space=pltpu.VMEM)
    results = pl.pallas_call(
        functools.partial(plane_kernel, lines, FORWARD, BACKWARD),
        out_shape=(
            vmem((rows, genes), F32),
            vmem((1, 1), F32),
            vmem((rows, cells), F32),
            vmem((cb, genes), F32),
        ),
        in_specs=[anywhere] * 6,
        out_specs=(in_vmem,) * 4,
        scratch_shapes=scratch,
        compiler_params=pltpu.CompilerParams(
            collective_id=0, has_side_effects=True, vmem_limit_bytes=48 * 1024 * 1024
        ),
    )(*map(in_hbm, (logits, expr, spatial, slide_spots, spot_cells, cell_prior.reshape(1, cells))))
    pred, loss, grad_logits, grad_expr = pl.pallas_call(
        deliver,
        out_shape=(
            jax.ShapeDtypeStruct((slides, slide_rows, genes), F32),
            jax.ShapeDtypeStruct((1, 1), F32),
            jax.ShapeDtypeStruct((slides, slide_rows, cells), F32),
            jax.ShapeDtypeStruct((cb, genes), F32),
        ),
        in_specs=[anywhere] * 4,
        out_specs=(anywhere,) * 4,
        scratch_shapes=[dma((2 * slides + 2,))],
        compiler_params=pltpu.CompilerParams(vmem_limit_bytes=4 * 1024 * 1024),
    )(*map(in_place, results))
    return pred, loss.reshape(()), grad_logits, grad_expr


def general_plan(logits, expr, spatial, slide_spots, spot_cells, cell_prior):
    place = lax.axis_index("spot")
    side = lax.axis_index("gene")
    rows_all = logits.shape[1]
    cell_rows = expr.shape[0]
    weights = cell_prior.astype(jnp.float32) / fixed_point
    gene_share = (place == 0).astype(jnp.float32)
    row_share = (side == 0).astype(jnp.float32)
    own_weights = lax.dynamic_slice_in_dim(weights, place * cell_rows, cell_rows, 0)
    expr_acc = jnp.zeros((cell_rows, expr.shape[1]), jnp.float32)
    loss_local = jnp.zeros((), jnp.float32)
    pred_list = []
    grad_list = []
    for slide in range(logits.shape[0]):
        logit_rows = logits[slide]
        counted = spot_cells[slide].astype(jnp.float32)
        target = spatial[slide]
        positions = place * rows_all + jnp.arange(rows_all, dtype=jnp.int32)
        valid = (positions < slide_spots[slide]).astype(jnp.float32)
        peak = jnp.max(logit_rows, axis=1, keepdims=True)
        raised = jnp.exp(logit_rows - peak)
        probs = raised / jnp.sum(raised, axis=1, keepdims=True)
        mass = jnp.dot(probs, weights, precision=lax.Precision.HIGHEST)
        blocks = lax.all_to_all(probs, "spot", split_axis=1, concat_axis=0, tiled=True)
        pred = lax.psum_scatter(
            jnp.dot(blocks, expr, precision=lax.Precision.HIGHEST),
            "spot",
            scatter_dimension=0,
            tiled=True,
        )
        gene_dot = jnp.sum(valid[:, None] * pred * target, axis=0)
        gene_pred = jnp.sum(valid[:, None] * pred * pred, axis=0)
        gene_true = jnp.sum(valid[:, None] * target * target, axis=0)
        mass_part = jnp.sum(valid * mass)
        kcell = valid * counted
        cell_part = jnp.sum(kcell)
        spot_dot = jnp.sum(pred * target, axis=1)
        spot_pred = jnp.sum(pred * pred, axis=1)
        spot_true = jnp.sum(target * target, axis=1)
        gene_dot, gene_pred, gene_true, mass_total, cell_total = lax.psum(
            (gene_dot, gene_pred, gene_true, mass_part, cell_part), "spot"
        )
        spot_dot, spot_pred, spot_true = lax.psum((spot_dot, spot_pred, spot_true), "gene")
        gene_inv = lax.rsqrt(gene_pred * gene_true + tiny)
        cos_gene = gene_dot * gene_inv
        spot_inv = lax.rsqrt(spot_pred * spot_true + tiny)
        cos_spot = spot_dot * spot_inv
        share = kcell / cell_total
        scale_count = slide_spots[slide].astype(jnp.float32)
        kl_part = jnp.sum(
            share * (jnp.log(counted) - jnp.log(cell_total) - jnp.log(mass) + jnp.log(mass_total))
        )
        loss_local = loss_local - gene_share * jnp.sum(cos_gene)
        loss_local = loss_local + row_share * (scale_count * kl_part - jnp.sum(valid * cos_spot))
        gene_back = cos_gene * gene_true / (gene_pred * gene_true + tiny)
        spot_back = cos_spot * spot_true / (spot_pred * spot_true + tiny)
        dpred = -valid[:, None] * (
            target * (gene_inv[None, :] + spot_inv[:, None])
            - pred * gene_back[None, :]
            - pred * spot_back[:, None]
        )
        dmass = scale_count * valid * (1.0 / mass_total - share / mass)
        pred_list.append(pred)
        grads_full, mass_full = (
            lax.all_gather(dpred, "spot", axis=0, tiled=True),
            lax.all_gather(dmass, "spot", axis=0, tiled=True),
        )
        dprob_cells = jnp.dot(grads_full, expr.T, precision=lax.Precision.HIGHEST)
        dprob_cells = lax.psum(dprob_cells, "gene")
        expr_acc = expr_acc + lax.dot_general(
            blocks, grads_full, (((0,), (0,)), ((), ())), precision=lax.Precision.HIGHEST
        )
        dprob_cells = dprob_cells + mass_full[:, None] * own_weights[None, :]
        dprob_rows = lax.all_to_all(dprob_cells, "spot", split_axis=0, concat_axis=1, tiled=True)
        inner = jnp.sum(probs * dprob_rows, axis=1, keepdims=True)
        dlogit = probs * (dprob_rows - inner)
        grad_list.append(dlogit)
    loss = lax.psum(loss_local, ("spot", "gene"))
    return (jnp.stack(pred_list), loss, jnp.stack(grad_list), expr_acc)


def solution(mesh):
    places = mesh.shape["spot"]

    def on_device(logits, expr, spatial, slide_spots, spot_cells, cell_prior):
        if places == PLANE * PLANE and mesh.shape["gene"] == 2 and expr.shape[1] == sum(FORWARD):
            return plane_call(
                logits, expr, spatial, slide_spots, spot_cells, cell_prior, places // PLANE
            )
        return general_plan(logits, expr, spatial, slide_spots, spot_cells, cell_prior)

    in_specs = (
        P(None, "spot", None),
        P("spot", "gene"),
        P(None, "spot", "gene"),
        P(),
        P(None, "spot"),
        P(),
    )
    out_specs = (P(None, "spot", "gene"), P(), P(None, "spot", None), P("spot", "gene"))
    return jax.shard_map(
        on_device, mesh=mesh, in_specs=in_specs, out_specs=out_specs, check_vma=False
    )
```

```python
import functools

import jax
import jax.numpy as jnp
from jax import lax
from jax.experimental import pallas as pl
from jax.experimental.pallas import tpu as pltpu
from jax.sharding import PartitionSpec as P

tiny = 1e-06
fixed_point = 16384.0
F32 = jnp.float32
BF16 = jnp.bfloat16
MESH = pl.DeviceIdType.MESH

PLANE = 4
LANES = 128
STEP_ROWS = 16
BLOCK = 32
TALL = 256
FORWARD = (128, 256, 256, 128, 128, 128)
BACKWARD = (128, 128, 256, 256, 256)
SPLIT = 2
LEAD = 1
NEAR_LEAD = 3
EARLY = 3
STEPS = (
    ("far", 0),
    ("far", 1),
    ("near", 0),
    ("share",),
    ("far", 2),
    ("far", 3),
    ("take",),
    ("whole", 0),
    ("near", 1),
    ("product", 0),
    ("sum", 0),
    ("whole", 1),
    ("near", 2),
    ("product", 1),
    ("whole", 2),
    ("product", 2),
    ("whole", 3),
    ("near", 3),
    ("product", 3),
    ("far", 4),
    ("whole", 4),
    ("near", 4),
    ("product", 4),
    ("sum", 1),
    ("turn", 0),
    ("far", 5),
    ("whole", 5),
    ("near", 5),
    ("product", 5),
    ("sum", 2),
    ("plane", 0),
    ("turn", 1),
    ("sum", 3),
    ("line", 0),
    ("sum", 4),
    ("sum", 5),
    ("plane", 1),
    ("cores",),
    ("genes", 0),
    ("spots",),
    ("grad", 0),
    ("grad", 1),
    ("line", 1),
    ("backward", 0),
    ("grad", 2),
    ("backward", 1),
    ("add_near", 0),
    ("genes", 1),
    ("grad", 3),
    ("backward", 2),
    ("probs", 0),
    ("add_far", 0),
    ("probs", 1),
    ("expr", 0),
    ("grad", 4),
    ("add_near", 1),
    ("probs", 2),
    ("terms",),
    ("backward", 3),
    ("probs", 3),
    ("add_near", 2),
    ("backward", 4),
    ("add_far", 1),
    ("probs", 4),
    ("exchange",),
    ("add_near", 3),
    ("add_far", 2),
    ("left",),
    ("return",),
    ("loss",),
    ("add_far", 3),
    ("expr", 1),
    ("add_near", 4),
    ("logits",),
    ("add_far", 4),
    ("expr", 2),
    ("expr", 3),
    ("expr", 4),
)


def halves(value):
    high = value.astype(BF16)
    return high, (value - high.astype(F32)).astype(BF16)


def threefold(value):
    high, low = halves(value)
    return jnp.concatenate([high, high, low], axis=1)


def product(a, b, contract):
    return lax.dot_general(a, b, (contract, ((), ())), preferred_element_type=F32)


def plane_kernel(lines, forward_widths, backward_widths, *refs):
    chunks, turns = len(forward_widths), len(backward_widths)
    (
        (logits_ref, expr_ref, spatial_ref, count_in, cells_in, prior_in),
        (pr, loss_ref, glog, ge),
        (count_ref, cells_ref, prior_ref, lg, lq, tg, ex, pq, ab, af, probs_3, turned_3, expr_3, sacc, s1, s2, gv, ss, rowv, rs),
        (grad_3, factor, t0, p0, vr, fs, fx, fy, fz, fr, inn, l1, l2),
        (loc, ou_s, ou_r, od_s, od_r, fu_s, fu_r, fd_s, fd_r, a_s, a_r, a2_s, a2_r, r_s, r_r),
        (c_s, c_r, s1_s, s1_r, s2_s, s2_r, ss_s, ss_r, d_s, d_r, ru_s, ru_r, rd_s, rd_r),
        (f_s, f_r, fx_s, fx_r, go_s, go_r, in_s, in_r, l1_s, l1_r, l2_s, l2_r, t0_s, t0_r, p0_s, p0_r, vr_s, vr_r),
        bb,
        cs,
        cr,
        ds,
        es,
        ru,
        rd,
    ) = grouped(refs, (6, 4, 20, 13, 15, 14, 18, chunks, chunks, chunks, turns, turns, turns, turns))
    place = lax.axis_index("spot")
    core = lax.axis_index("gene")
    z = place // PLANE
    q = place % PLANE
    col, row = q % 2, q // 2
    mates = ((1 - row) * 2 + 1 - col, row * 2 + 1 - col, (1 - row) * 2 + col)
    others = tuple((z + step) % lines for step in range(1, lines))
    up, down = (place + PLANE, core), (place - PLANE, core)
    sibling = (place, 1 - core)
    slides, slide_rows = logits_ref.shape[0], logits_ref.shape[1]
    rows = slides * slide_rows
    cb = expr_ref.shape[0]
    genes = expr_ref.shape[1]
    last = lines - 1

    def mate(p):
        return (z * PLANE + p, core)

    def send(src, dst, send_sem, recv_sem, device):
        copy = pltpu.make_async_remote_copy(
            src_ref=src, dst_ref=dst, send_sem=send_sem, recv_sem=recv_sem, device_id=device, device_id_type=MESH
        )
        copy.start()

    def arrived(dst, recv_sem):
        pltpu.make_async_copy(dst, dst, recv_sem).wait()

    sent = arrived

    def cols(k):
        return pl.ds(sum(forward_widths[:k]), forward_widths[k])

    def turn_cols(k):
        return pl.ds(sum(backward_widths[:k]), backward_widths[k])

    def block(index):
        return pl.ds(pl.multiple_of(index * cb, cb), cb)

    def share(index):
        return pl.ds(pl.multiple_of(index * rows, rows), rows)

    def half(index):
        return pl.ds(pl.multiple_of(index * slide_rows, slide_rows), slide_rows)

    small = ((prior_in, prior_ref), (count_in, count_ref), (cells_in, cells_ref))
    pltpu.make_async_copy(expr_ref, ex, loc.at[2 * slides]).start()
    for m in range(slides):
        pltpu.make_async_copy(logits_ref.at[m], lg.at[half(m)], loc.at[m]).start()
    for at, (src, dst) in enumerate(small):
        pltpu.make_async_copy(src, dst, loc.at[2 * slides + 1 + at]).start()
    for m in range(slides):
        pltpu.make_async_copy(spatial_ref.at[m], tg.at[half(m)], loc.at[slides + m]).start()

    barrier = pltpu.get_barrier_semaphore()
    for p in mates:
        pl.semaphore_signal(barrier, inc=1, device_id=mate(p), device_id_type=MESH)
    for o in others:
        pl.semaphore_signal(barrier, inc=1, device_id=(o * PLANE + q, core), device_id_type=MESH)
    pl.semaphore_signal(barrier, inc=1, device_id=sibling, device_id_type=MESH)
    pltpu.make_async_copy(expr_ref, ex, loc.at[2 * slides]).wait()
    for k in range(chunks):
        bb[k][block(z), :] = ex[:, cols(k)]
    for m in range(slides):
        pltpu.make_async_copy(logits_ref.at[m], lg.at[half(m)], loc.at[m]).wait()
    for p in range(PLANE):
        for line in range(lines):
            lq[p, :, pl.ds(line * cb, cb)] = lg[half(core), pl.ds((line * PLANE + p) * cb, cb)]
    pl.semaphore_wait(barrier, len(mates) + len(others) + 1)

    def own_up(k):
        here = bb[k].at[block(z)]
        send(here, here, ou_s.at[k], ou_r.at[k], up)

    def own_down(k):
        here = bb[k].at[block(z)]
        send(here, here, od_s.at[k], od_r.at[k], down)

    def low(at):
        return 2 * at < lines

    for at in range(lines):

        @pl.when(z == at)
        def _():
            for k in range(chunks):
                if at < last and (at == 0 or k < (LEAD if low(at) else NEAR_LEAD)):
                    own_up(k)
                if at > 0 and (at == last or k < (NEAR_LEAD if low(at) else LEAD)):
                    own_down(k)

    for p in mates:
        send(lq.at[p], ab.at[q, half(core)], a_s, a_r.at[q], mate(p))

    def from_below(k, at):
        arrived(bb[k].at[pl.ds((at - 1) * cb, cb)], ou_r.at[k])
        if at > 1:
            arrived(bb[k].at[pl.ds(0, (at - 1) * cb)], fu_r.at[k])

    def from_above(k, at):
        arrived(bb[k].at[pl.ds((at + 1) * cb, cb)], od_r.at[k])
        if at < last - 1:
            arrived(bb[k].at[pl.ds((at + 2) * cb, (last - 1 - at) * cb)], fd_r.at[k])

    def upward(k, at):
        from_below(k, at)
        here = bb[k].at[pl.ds(0, at * cb)]
        send(here, here, fu_s.at[k], fu_r.at[k], up)

    def downward(k, at):
        from_above(k, at)
        here = bb[k].at[pl.ds((at + 1) * cb, (last - at) * cb)]
        send(here, here, fd_s.at[k], fd_r.at[k], down)

    def forward_far(k):
        for at in range(1, last):

            @pl.when(z == at)
            def _():
                (upward if low(at) else downward)(k, at)
                if k + LEAD < chunks:
                    (own_up if low(at) else own_down)(k + LEAD)

    def forward_near(k):
        for at in range(1, last):

            @pl.when(z == at)
            def _():
                (downward if low(at) else upward)(k, at)
                if k + NEAR_LEAD < chunks:
                    (own_down if low(at) else own_up)(k + NEAR_LEAD)

    def gathered(k):
        @pl.when(z == 0)
        def _():
            from_above(k, 0)

        @pl.when(z == last)
        def _():
            from_below(k, last)

    for at, (src, dst) in enumerate(small):
        pltpu.make_async_copy(src, dst, loc.at[2 * slides + 1 + at]).wait()
    weights = prior_ref[...].astype(F32) / fixed_point

    @pl.loop(0, rows // STEP_ROWS)
    def _(step):
        at = pl.ds(pl.multiple_of(step * STEP_ROWS, STEP_ROWS), STEP_ROWS)
        value = lg[at, :]
        peak = jnp.max(value, axis=1, keepdims=True)
        raised = jnp.exp(value - peak)
        scale = 1.0 / jnp.sum(raised, axis=1, keepdims=True)
        probs = raised * scale
        mass_rows = jnp.sum(probs * weights, axis=1, keepdims=True)
        rowv[0, at, :] = jnp.broadcast_to(mass_rows, (STEP_ROWS, LANES))
        rowv[1, at, :] = jnp.broadcast_to(peak, (STEP_ROWS, LANES))
        rowv[2, at, :] = jnp.broadcast_to(scale, (STEP_ROWS, LANES))
        for p in range(PLANE):
            for line in range(lines):
                at_cells = (line * PLANE + p) * cb
                pq[p, at, pl.ds(line * cb, cb)] = probs[:, at_cells : at_cells + cb]

    wide = lax.broadcasted_iota(jnp.int32, (rows, LANES), 1)
    rs[q] = jnp.where(wide == 0, rowv[1], rowv[2]).T[0:8]
    for p in mates:
        send(rs.at[q], rs.at[q], r_s, r_r.at[q], mate(p))

    rid = lax.broadcasted_iota(jnp.int32, (rows, 1), 0)
    first = rid < slide_rows
    position = place * slide_rows + jnp.where(first, rid, rid - slide_rows)
    count = jnp.where(first, count_ref[0], count_ref[1])
    valid = (position < count).astype(F32)
    scale_count = count.astype(F32)
    square = (slide_rows, slide_rows)
    eye = lax.broadcasted_iota(jnp.int32, square, 0) == lax.broadcasted_iota(jnp.int32, square, 1)
    counted = jnp.concatenate(
        [
            jnp.sum(jnp.where(eye, cells_ref[m : m + 1, :].astype(F32), 0.0), axis=1, keepdims=True)
            for m in range(slides)
        ],
        axis=0,
    )
    mass = rowv[0, :, 0:1]
    kcell = valid * counted

    def by_slide(value):
        return [jnp.sum(value[m * slide_rows : (m + 1) * slide_rows], axis=0, keepdims=True) for m in range(slides)]

    mass_parts = by_slide(valid * mass)
    cell_parts = by_slide(kcell)
    lane = lax.broadcasted_iota(jnp.int32, (1, LANES), 1)
    scalars = jnp.zeros((1, LANES), F32)
    for at, value in enumerate(mass_parts + cell_parts):
        scalars = jnp.where(lane == at, value, scalars)
    for m in range(slides):
        pltpu.make_async_copy(spatial_ref.at[m], tg.at[half(m)], loc.at[slides + m]).wait()

    head = backward_widths[0]
    t0[q] = tg[:, 0:head]
    for p in mates:
        send(t0.at[q], t0.at[q], t0_s, t0_r.at[q], mate(p))
    sacc[...] = jnp.zeros_like(sacc)
    s1[q, 3 * slides :, :] = jnp.zeros((8 - 3 * slides, genes), F32)
    s1[q, 3 * slides : 3 * slides + 1, 0:LANES] = scalars

    def share_logits():
        for p in (mates[1], mates[2], mates[0]):
            here = ab.at[p, half(core)]
            arrived(here, a_r.at[p])
            send(here, here, a2_s, a2_r.at[p], sibling)

    def lay_probs(p, at, value):
        af[p, at, :] = value
        there = pl.ds(pl.multiple_of(p * rows + at.start, BLOCK), BLOCK)
        probs_3[there, :] = threefold(value)

    def take_probs():
        in_blocks(0, rows, lambda at: lay_probs(q, at, pq[q, at, :]))
        for p in (mates[1], mates[2], mates[0]):
            arrived(rs.at[p], r_r.at[p])
            arrived(ab.at[p, half(1 - core)], a2_r.at[p])
            rowv[1] = jnp.concatenate([rs[p].T, jnp.zeros((rows, LANES - 8), F32)], axis=1)

            def take(at):
                probs = jnp.exp(ab[p, at, :] - rowv[1, at, 0:1]) * rowv[1, at, 1:2]
                lay_probs(p, at, probs)

            in_blocks(0, rows, take)

    def transpose(part):
        @pl.loop(0, PLANE // 2)
        def _(step):
            p = part * (PLANE // 2) + step
            high, low_part = halves(af[p].T)
            for third, value in enumerate((high, high, low_part)):
                turned_3[:, pl.ds(pl.multiple_of(third * PLANE * rows + p * rows, rows), rows)] = value

    def in_blocks(start, count, body):
        @pl.loop(0, count // BLOCK)
        def _(step):
            body(pl.ds(pl.multiple_of(start + step * BLOCK, BLOCK), BLOCK))

    quarter = lines * cb

    def lay_factor(at, length, width, value):
        high, low_part = halves(value)
        for third, part in enumerate((high, low_part, high)):
            here = pl.ds(pl.multiple_of(third * length + at.start, BLOCK), BLOCK)
            factor[here, 0:width] = part

    def keep_expr(k, at, value):
        start = sum(forward_widths[:k])
        for turn in range(turns):
            origin, width = sum(backward_widths[:turn]), backward_widths[turn]
            lo, hi = max(start, origin), min(start + forward_widths[k], origin + width)
            if lo < hi:
                high, low_part = halves(value[:, lo - start : hi - start])
                for third, part in enumerate((high, low_part, high)):
                    expr_3[at, pl.ds(3 * origin + third * width + lo - origin, hi - lo)] = part

    def three_turn_cols(k):
        return pl.ds(3 * sum(backward_widths[:k]), 3 * backward_widths[k])

    def forward_product(k):
        width = forward_widths[k]

        def lay(at):
            value = bb[k][at, :]
            lay_factor(at, quarter, width, value)
            keep_expr(k, at, value)

        in_blocks(0, quarter, lay)
        if k < chunks - 1:

            @pl.loop(0, PLANE * rows // TALL)
            def _(step):
                tall = pl.ds(pl.multiple_of(step * TALL, TALL), TALL)
                cs[k][tall, :] = product(probs_3[tall, :], factor[0 : 3 * quarter, 0:width], ((1,), (0,)))

            for p in mates:
                pass_pred(k, p)
        else:
            for side, served in ((1 - row, (mates[0], mates[2])), (row, (mates[1],))):
                pair = pl.ds(pl.multiple_of(2 * side * rows, 2 * rows), 2 * rows)
                cs[k][pair, :] = product(probs_3[pair, :], factor[0 : 3 * quarter, 0:width], ((1,), (0,)))
                for p in served:
                    pass_pred(k, p)

    def pass_pred(k, p):
        send(cs[k].at[share(p)], cr[k].at[q], c_s.at[k], c_r.at[k, q], mate(p))

    def finish_pred(k):
        total = cs[k][share(q), :]
        for p in mates:
            arrived(cr[k].at[p], c_r.at[k, p])
            total = total + cr[k][p]
        pr[:, cols(k)] = total
        if k == 0:
            p0[q] = total[:, 0:head]
            for p in mates:
                send(p0.at[q], p0.at[q], p0_s, p0_r.at[q], mate(p))
        truth = tg[:, cols(k)]
        for at, value in enumerate((total * truth, total * total, truth * truth)):
            sacc[at] += lane_groups(value)
        kept = valid * total
        stats = by_slide(kept * truth) + by_slide(kept * total) + by_slide(valid * truth * truth)
        s1[q, 0 : 3 * slides, cols(k)] = jnp.concatenate(stats, axis=0)

    early = sum(forward_widths[:EARLY])
    parts = (pl.ds(0, early), pl.ds(early, genes - early))

    def sum_plane(at):
        for p in mates:
            send(s1.at[q, :, parts[at]], s1.at[q, :, parts[at]], s1_s, s1_r.at[at, q], mate(p))

    def sum_line(at):
        for p in mates:
            arrived(s1.at[p, :, parts[at]], s1_r.at[at, p])
        s2[z, :, parts[at]] = (s1[0, :, parts[at]] + s1[1, :, parts[at]]) + (s1[2, :, parts[at]] + s1[3, :, parts[at]])
        for o in others:
            send(s2.at[z, :, parts[at]], s2.at[z, :, parts[at]], s2_s, s2_r.at[at, z], (o * PLANE + q, core))

    kept = {}

    def finish_genes(at):
        for o in others:
            arrived(s2.at[o, :, parts[at]], s2_r.at[at, o])
        total = s2[0, :, parts[at]]
        for line in range(1, lines):
            total = total + s2[line, :, parts[at]]
        gene_dot, gene_pred, gene_true = total[0:2], total[2:4], total[4:6]
        gene_inv = lax.rsqrt(gene_pred * gene_true + tiny)
        cos_gene = gene_dot * gene_inv
        gv[0:2, parts[at]] = gene_inv
        gv[2:4, parts[at]] = cos_gene * gene_true / (gene_pred * gene_true + tiny)
        kept["genes", at] = jnp.sum(jnp.sum(cos_gene, axis=1, keepdims=True), axis=0, keepdims=True)
        if at == 0:
            kept["mass"] = jnp.where(first, total[6:7, 0:1], total[6:7, 1:2])
            kept["cells"] = jnp.where(first, total[6:7, 2:3], total[6:7, 3:4])

    def sum_cores():
        sums = [jnp.sum(sacc[at], axis=1, keepdims=True) for at in range(3)]
        ss[core] = jnp.where(wide == 0, sums[0], jnp.where(wide == 1, sums[1], sums[2])).T[0:8]
        send(ss.at[core], ss.at[core], ss_s, ss_r, sibling)

    def finish_spots():
        lane_id = lax.broadcasted_iota(jnp.int32, (1, rows), 1)
        first_lane = lane_id < slide_rows
        lane_position = place * slide_rows + jnp.where(first_lane, lane_id, lane_id - slide_rows)
        lane_valid = (lane_position < jnp.where(first_lane, count_ref[0], count_ref[1])).astype(F32)
        arrived(ss.at[1 - core], ss_r)
        spot = ss[0] + ss[1]
        spot_dot, spot_pred, spot_true = spot[0:1], spot[1:2], spot[2:3]
        spot_inv = lax.rsqrt(spot_pred * spot_true + tiny)
        cos_spot = spot_dot * spot_inv
        spot_back = cos_spot * spot_true / (spot_pred * spot_true + tiny)
        kept["cos"] = jnp.sum(lane_valid * cos_spot, axis=1, keepdims=True)
        vectors = [lane_valid * spot_inv, lane_valid * spot_back, lane_valid, jnp.zeros((5, rows), F32)]
        vr[q] = jnp.concatenate(vectors, axis=0)
        sacc[0] = jnp.zeros_like(sacc[0])

    def gradient(truth, guess, by_row, k):
        pieces = []
        for m in range(slides):
            lo, hi = m * slide_rows, (m + 1) * slide_rows
            inverse, back = gv[m : m + 1, turn_cols(k)], gv[2 + m : 3 + m, turn_cols(k)]
            spot_inv, spot_back, spot_valid = by_row[lo:hi, 0:1], by_row[lo:hi, 1:2], by_row[lo:hi, 2:3]
            pieces.append(
                guess[lo:hi] * (spot_valid * back + spot_back) - truth[lo:hi] * (spot_valid * inverse + spot_inv)
            )
        return jnp.concatenate(pieces, axis=0)

    def head_gradient():
        for p in mates:
            arrived(t0.at[p], t0_r.at[p])
            arrived(p0.at[p], p0_r.at[p])
            arrived(vr.at[p], vr_r.at[p])
        for p in range(PLANE):
            ds[0][share(p), :] = gradient(t0[p], p0[p], vr[p].T, 0)
        sacc[0] += lane_groups(ds[0][share(q), :] * p0[q])

    def send_grad(k):
        if k == 0:
            for p in mates:
                send(vr.at[q], vr.at[q], vr_s, vr_r.at[q], mate(p))
            kept["by_row"] = vr[q].T
            return
        grad = gradient(tg[:, turn_cols(k)], pr[:, turn_cols(k)], kept["by_row"], k)
        here = ds[k].at[share(q)]
        here[...] = grad
        for p in mates:
            send(here, here, d_s.at[k], d_r.at[k, q], mate(p))
        sacc[0] += lane_groups(grad * pr[:, turn_cols(k)])

    def send_terms():
        mass_total, cell_total = kept["mass"], kept["cells"]
        portion = kcell / cell_total
        kl_rows = portion * (jnp.log(counted) - jnp.log(cell_total) - jnp.log(mass) + jnp.log(mass_total))
        dmass = scale_count * valid * (1.0 / mass_total - portion / mass)
        terms = jnp.sum(scale_count * kl_rows, axis=0, keepdims=True) - kept["cos"]
        l1[q] = jnp.broadcast_to(terms, (8, LANES))
        for p in mates:
            send(l1.at[q], l1.at[q], l1_s, l1_r.at[q], mate(p))
        inner = jnp.sum(sacc[0], axis=1, keepdims=True)
        inn[core] = jnp.where(wide == 0, inner, kept["genes", 0] + kept["genes", 1])
        send(inn.at[core], inn.at[core], in_s, in_r, sibling)
        rowv[1] = jnp.broadcast_to(dmass, (rows, LANES))

    middle = lines // 2

    def backward_product(k):
        if k == 0:
            head_gradient()
        else:
            for p in mates:
                arrived(ds[k].at[share(p)], d_r.at[k, p])
        width, spots = backward_widths[k], PLANE * rows

        def lay(at):
            value = ds[k][at, :]
            lay_factor(at, spots, width, value)
            grad_3[at, three_turn_cols(k)] = threefold(value)

        in_blocks(0, spots, lay)
        if not halved(k):

            @pl.loop(0, quarter // TALL)
            def _(step):
                tall = pl.ds(pl.multiple_of(step * TALL, TALL), TALL)
                es[k][tall, :] = product(turned_3[tall, :], factor[0 : 3 * spots, 0:width], ((1,), (0,)))

        for turn in range(2):
            if halved(k):
                side = (1 - z // middle) if turn == 0 else z // middle
                pair = pl.ds(pl.multiple_of(side * middle * cb, middle * cb), middle * cb)
                es[k][pair, :] = product(turned_3[pair, :], factor[0 : 3 * spots, 0:width], ((1,), (0,)))

            @pl.when(z == 0)
            def _():
                if halved(k):
                    pass_up(k, middle if turn == 0 else 1, middle if turn == 0 else middle - 1, turn)
                elif whole(k):
                    if turn == 0:
                        pass_up(k, 1, last, 0)
                elif turn == 0:
                    for line in range(last, 0, -1):
                        pass_up(k, line, 1, line)

            @pl.when(z == last)
            def _():
                if halved(k):
                    pass_down(k, 0 if turn == 0 else middle, middle if turn == 0 else middle - 1, turn)
                elif whole(k):
                    if turn == 0:
                        pass_down(k, 0, last, 0)
                elif turn == 0:
                    for line in range(last):
                        pass_down(k, line, 1, line)

    def halved(k):
        return k == 0

    def whole(k):
        return 0 < k < turns - SPLIT

    def pass_up(k, line, count, slot):
        here = pl.ds(line * cb, count * cb)
        send(es[k].at[here], ru[k].at[here], ru_s.at[k], ru_r.at[k, slot], up)

    def pass_down(k, line, count, slot):
        here = pl.ds(line * cb, count * cb)
        send(es[k].at[here], rd[k].at[here], rd_s.at[k], rd_r.at[k, slot], down)

    def take_up(k, line, count, slot):
        arrived(ru[k].at[pl.ds(line * cb, count * cb)], ru_r.at[k, slot])

    def take_down(k, line, count, slot):
        arrived(rd[k].at[pl.ds(line * cb, count * cb)], rd_r.at[k, slot])

    def add_up(k, line, count):
        def add(at):
            es[k][at, :] += ru[k][at, :]

        in_blocks(line * cb, count * cb, add)

    def add_down(k, line, count):
        def add(at):
            es[k][at, :] += rd[k][at, :]

        in_blocks(line * cb, count * cb, add)

    def rising(k, at):
        if halved(k) or whole(k):
            start = middle if halved(k) else at
            take_up(k, start, lines - start, 0)
            above = max(at + 1, start)
            add_up(k, above, lines - above)
            pass_up(k, above, lines - above, 0)
        else:
            for line in range(last, at, -1):
                take_up(k, line, 1, line)
                add_up(k, line, 1)
                pass_up(k, line, 1, line)

    def falling(k, at):
        if halved(k) or whole(k):
            end = middle if halved(k) else at + 1
            take_down(k, 0, end, 0)
            below = min(at, end)
            add_down(k, 0, below)
            pass_down(k, 0, below, 0)
        else:
            for line in range(at):
                take_down(k, line, 1, line)
                add_down(k, line, 1)
                pass_down(k, line, 1, line)

    def add_near(k):
        for at in range(1, last):

            @pl.when(z == at)
            def _():
                (rising if low(at) else falling)(k, at)

    def add_far(k):
        for at in range(1, last):

            @pl.when(z == at)
            def _():
                (falling if low(at) else rising)(k, at)

    def finish_expr(k):
        for at in range(lines):

            @pl.when(z == at)
            def _():
                if at > 0:
                    if halved(k) and at < middle:
                        take_up(k, at, 1, 1)
                    elif at == last and (halved(k) or whole(k)):
                        take_up(k, at, 1, 0)
                    elif not halved(k) and not whole(k):
                        take_up(k, at, 1, at)
                if at < last:
                    if halved(k) and at >= middle:
                        take_down(k, at, 1, 1)
                    elif at == 0 and (halved(k) or whole(k)):
                        take_down(k, at, 1, 0)
                    elif not halved(k) and not whole(k):
                        take_down(k, at, 1, at)

        from_low, from_high = z > 0, z < last

        @pl.loop(0, cb // BLOCK)
        def _(step):
            here = pl.ds(pl.multiple_of(step * BLOCK, BLOCK), BLOCK)
            own = pl.ds(pl.multiple_of(z * cb + step * BLOCK, BLOCK), BLOCK)
            total = es[k][own, :]
            total = total + jnp.where(from_low, ru[k][own, :], 0.0)
            ge[here, turn_cols(k)] = total + jnp.where(from_high, rd[k][own, :], 0.0)

    def probs_gradient(k):
        at = three_turn_cols(k)

        @pl.loop(0, PLANE * rows // TALL)
        def _(step):
            tall = pl.ds(pl.multiple_of(step * TALL, TALL), TALL)
            part = product(grad_3[tall, at], expr_3[:, at], ((1,), (1,)))
            if k == 0:
                fs[tall, :] = part
            else:
                fs[tall, :] += part

    def slide_of(p, m):
        return pl.ds(pl.multiple_of(p * rows + m * slide_rows, slide_rows), slide_rows)

    def sum_probs_cores():
        for p in mates + (q,):
            fx[p] = fs[slide_of(p, 1 - core), :]
            send(fx.at[p], fy.at[p], fx_s, fx_r.at[p], sibling)

    def return_probs():
        for p in mates:
            arrived(fy.at[p], fx_r.at[p])
            fz[p] = fs[slide_of(p, core), :] + fy[p]
            send(fz.at[p], fr.at[q], f_s, f_r.at[q], mate(p))
        arrived(fy.at[q], fx_r.at[q])
        fr[q] = fs[slide_of(q, core), :] + fy[q]

    def pass_terms():
        for p in mates:
            arrived(l1.at[p], l1_r.at[p])
        l2[z] = (l1[0] + l1[1]) + (l1[2] + l1[3])
        for o in others:
            send(l2.at[z], l2.at[z], l2_s, l2_r.at[z], (o * PLANE + q, core))

    def part_of(slide, m):
        start = slide * slide_rows + m * (slide_rows // 2)
        return pl.ds(pl.multiple_of(start, slide_rows // 2), slide_rows // 2)

    def finish_logits():
        arrived(inn.at[1 - core], in_r)
        rowv[2] = (inn[0] + inn[1]) + rowv[1] * rowv[0]
        for p in mates:
            arrived(fr.at[p], f_r.at[p])
        for m in range(2):

            @pl.loop(0, slide_rows // STEP_ROWS // 2)
            def _(step):
                row_at = (m * (slide_rows // STEP_ROWS // 2) + step) * STEP_ROWS
                at = pl.ds(pl.multiple_of(row_at, STEP_ROWS), STEP_ROWS)
                whole_at = pl.ds(pl.multiple_of(core * slide_rows + row_at, STEP_ROWS), STEP_ROWS)
                by_mass, total_inner = rowv[1, whole_at, 0:1], rowv[2, whole_at, 0:1]
                for p in range(PLANE):
                    for line in range(lines):
                        here, there = pl.ds(line * cb, cb), (line * PLANE + p) * cb
                        grad = fr[p, at, here] + by_mass * weights[:, there : there + cb]
                        glog[whole_at, pl.ds(there, cb)] = pq[p, whole_at, here] * (grad - total_inner)

            here = part_of(core, m)
            send(glog.at[here], glog.at[here], go_s, go_r.at[m], sibling)

    def forward_left():
        for k in range(chunks):

            @pl.when(z < last)
            def _():
                sent(bb[k].at[block(z)], ou_s.at[k])

            @pl.when(z > 0)
            def _():
                sent(bb[k].at[block(z)], od_s.at[k])

            for at in range(1, last):

                @pl.when(z == at)
                def _():
                    sent(bb[k].at[pl.ds(0, at * cb)], fu_s.at[k])
                    sent(bb[k].at[pl.ds((at + 1) * cb, (last - at) * cb)], fd_s.at[k])

        three = pl.ds(0, len(mates))
        sent(ab.at[three, half(0)], a_s)
        sent(ab.at[three, half(0)], a2_s)
        sent(rs.at[three], r_s)
        sent(t0.at[three], t0_s)
        sent(p0.at[three], p0_s)
        for k in range(chunks):
            sent(cr[k].at[three], c_s.at[k])
        sent(s1.at[three], s1_s)
        sent(s2.at[pl.ds(0, last)], s2_s)
        sent(ss.at[0], ss_s)

    steps = {
        "far": forward_far,
        "near": forward_near,
        "share": share_logits,
        "take": take_probs,
        "whole": gathered,
        "product": forward_product,
        "sum": finish_pred,
        "turn": transpose,
        "plane": sum_plane,
        "line": sum_line,
        "genes": finish_genes,
        "cores": sum_cores,
        "spots": finish_spots,
        "grad": send_grad,
        "terms": send_terms,
        "backward": backward_product,
        "probs": probs_gradient,
        "exchange": sum_probs_cores,
        "return": return_probs,
        "loss": pass_terms,
        "logits": finish_logits,
        "add_near": add_near,
        "add_far": add_far,
        "expr": finish_expr,
        "left": forward_left,
    }
    for name, *where in STEPS:
        steps[name](*where)

    for o in others:
        arrived(l2.at[o], l2_r.at[o])
    loss = l2[0]
    for line in range(1, lines):
        loss = loss + l2[line]
    loss_ref[...] = loss[0:1, 0:1] - (inn[0, 0:1, 1:2] + inn[1, 0:1, 1:2])
    for m in range(2):
        arrived(glog.at[part_of(1 - core, m)], go_r.at[m])

    for k in range(turns):
        for at in range(lines):

            @pl.when(z == at)
            def _():
                if at < last:
                    sent(es[k].at[pl.ds((at + 1) * cb, (last - at) * cb)], ru_s.at[k])
                if at > 0:
                    sent(es[k].at[pl.ds(0, at * cb)], rd_s.at[k])

    three = pl.ds(0, len(mates))
    for k in range(1, turns):
        sent(ds[k].at[pl.ds(0, len(mates) * rows)], d_s.at[k])
    sent(vr.at[three], vr_s)
    sent(inn.at[0], in_s)
    sent(l1.at[three], l1_s)
    sent(l2.at[pl.ds(0, last)], l2_s)
    sent(fr.at[three], f_s)
    sent(fx, fx_s)
    sent(glog.at[half(0)], go_s)


def lane_groups(value):
    parts = [value[:, at : at + LANES] for at in range(0, value.shape[1], LANES)]
    return functools.reduce(lambda a, b: a + b, parts)


def grouped(refs, sizes):
    at = 0
    for size in sizes:
        yield refs[at : at + size]
        at += size


def deliver(pred_in, loss_in, glog_in, gexp_in, pred_ref, loss_ref, glog_ref, gexp_ref, sems):
    slides, slide_rows = pred_ref.shape[0], pred_ref.shape[1]
    pairs = [(gexp_in, gexp_ref), (loss_in, loss_ref)]
    for m in range(slides):
        part = pl.ds(m * slide_rows, slide_rows)
        pairs += [(glog_in.at[part], glog_ref.at[m]), (pred_in.at[part], pred_ref.at[m])]
    copies = [pltpu.make_async_copy(src, dst, sems.at[at]) for at, (src, dst) in enumerate(pairs)]
    for copy in copies:
        copy.start()
    for copy in copies:
        copy.wait()


def plane_call(logits, expr, spatial, slide_spots, spot_cells, cell_prior, lines):
    slides, slide_rows, cells = logits.shape
    rows = slides * slide_rows
    cb, genes = expr.shape
    quarter = lines * cb
    spots = PLANE * rows
    chunks, turns = len(FORWARD), len(BACKWARD)
    dma = pltpu.SemaphoreType.DMA
    vmem = pltpu.VMEM
    anywhere = pl.BlockSpec(memory_space=pl.ANY)
    in_vmem = pl.BlockSpec(memory_space=pltpu.VMEM)
    scratch = [
        pltpu.SMEM((slides,), jnp.int32),
        vmem((slides, slide_rows), jnp.int32),
        vmem((1, cells), jnp.int32),
        vmem((rows, cells), F32),
        vmem((PLANE, slide_rows, quarter), F32),
        vmem((rows, genes), F32),
        vmem((cb, genes), F32),
        vmem((PLANE, rows, quarter), F32),
        vmem((PLANE, rows, quarter), F32),
        vmem((PLANE, rows, quarter), F32),
        vmem((spots, 3 * quarter), BF16),
        vmem((quarter, 3 * spots), BF16),
        vmem((quarter, 3 * genes), BF16),
        vmem((3, rows, LANES), F32),
        vmem((PLANE, 8, genes), F32),
        vmem((lines, 8, genes), F32),
        vmem((8, genes), F32),
        vmem((2, 8, rows), F32),
        vmem((3, rows, LANES), F32),
        vmem((PLANE, 8, rows), F32),
        vmem((spots, 3 * genes), BF16),
        vmem((3 * max(quarter, spots), max(FORWARD + BACKWARD)), BF16),
        vmem((PLANE, rows, BACKWARD[0]), F32),
        vmem((PLANE, rows, BACKWARD[0]), F32),
        vmem((PLANE, 8, rows), F32),
        vmem((spots, quarter), F32),
        vmem((PLANE, slide_rows, quarter), F32),
        vmem((PLANE, slide_rows, quarter), F32),
        vmem((PLANE, slide_rows, quarter), F32),
        vmem((PLANE, slide_rows, quarter), F32),
        vmem((2, rows, LANES), F32),
        vmem((PLANE, 8, LANES), F32),
        vmem((lines, 8, LANES), F32),
        dma((2 * slides + 4,)),
        dma((chunks,)),
        dma((chunks,)),
        dma((chunks,)),
        dma((chunks,)),
        dma((chunks,)),
        dma((chunks,)),
        dma((chunks,)),
        dma((chunks,)),
        dma,
        dma((PLANE,)),
        dma,
        dma((PLANE,)),
        dma,
        dma((PLANE,)),
        dma((chunks,)),
        dma((chunks, PLANE)),
        dma,
        dma((2, PLANE)),
        dma,
        dma((2, lines)),
        dma,
        dma,
        dma((turns,)),
        dma((turns, PLANE)),
        dma((turns,)),
        dma((turns, lines)),
        dma((turns,)),
        dma((turns, lines)),
        dma,
        dma((PLANE,)),
        dma,
        dma((PLANE,)),
        dma,
        dma((2,)),
        dma,
        dma,
        dma,
        dma((PLANE,)),
        dma,
        dma((lines,)),
        dma,
        dma((PLANE,)),
        dma,
        dma((PLANE,)),
        dma,
        dma((PLANE,)),
    ]
    for shape, widths in (
        ((quarter,), FORWARD),
        ((spots,), FORWARD),
        ((PLANE, rows), FORWARD),
        ((spots,), BACKWARD),
        ((quarter,), BACKWARD),
        ((quarter,), BACKWARD),
        ((quarter,), BACKWARD),
    ):
        scratch += [vmem(shape + (width,), F32) for width in widths]
    in_hbm = functools.partial(pltpu.with_memory_space_constraint, memory_space=pltpu.HBM)
    in_place = functools.partial(pltpu.with_memory_space_constraint, memory_space=pltpu.VMEM)
    results = pl.pallas_call(
        functools.partial(plane_kernel, lines, FORWARD, BACKWARD),
        out_shape=(
            vmem((rows, genes), F32),
            vmem((1, 1), F32),
            vmem((rows, cells), F32),
            vmem((cb, genes), F32),
        ),
        in_specs=[anywhere] * 6,
        out_specs=(in_vmem,) * 4,
        scratch_shapes=scratch,
        compiler_params=pltpu.CompilerParams(
            collective_id=0, has_side_effects=True, vmem_limit_bytes=48 * 1024 * 1024
        ),
    )(*map(in_hbm, (logits, expr, spatial, slide_spots, spot_cells, cell_prior.reshape(1, cells))))
    pred, loss, grad_logits, grad_expr = pl.pallas_call(
        deliver,
        out_shape=(
            jax.ShapeDtypeStruct((slides, slide_rows, genes), F32),
            jax.ShapeDtypeStruct((1, 1), F32),
            jax.ShapeDtypeStruct((slides, slide_rows, cells), F32),
            jax.ShapeDtypeStruct((cb, genes), F32),
        ),
        in_specs=[anywhere] * 4,
        out_specs=(anywhere,) * 4,
        scratch_shapes=[dma((2 * slides + 2,))],
        compiler_params=pltpu.CompilerParams(vmem_limit_bytes=4 * 1024 * 1024),
    )(*map(in_place, results))
    return pred, loss.reshape(()), grad_logits, grad_expr


def general_plan(logits, expr, spatial, slide_spots, spot_cells, cell_prior):
    place = lax.axis_index("spot")
    side = lax.axis_index("gene")
    rows_all = logits.shape[1]
    cell_rows = expr.shape[0]
    weights = cell_prior.astype(jnp.float32) / fixed_point
    gene_share = (place == 0).astype(jnp.float32)
    row_share = (side == 0).astype(jnp.float32)
    own_weights = lax.dynamic_slice_in_dim(weights, place * cell_rows, cell_rows, 0)
    expr_acc = jnp.zeros((cell_rows, expr.shape[1]), jnp.float32)
    loss_local = jnp.zeros((), jnp.float32)
    pred_list = []
    grad_list = []
    for slide in range(logits.shape[0]):
        logit_rows = logits[slide]
        counted = spot_cells[slide].astype(jnp.float32)
        target = spatial[slide]
        positions = place * rows_all + jnp.arange(rows_all, dtype=jnp.int32)
        valid = (positions < slide_spots[slide]).astype(jnp.float32)
        peak = jnp.max(logit_rows, axis=1, keepdims=True)
        raised = jnp.exp(logit_rows - peak)
        probs = raised / jnp.sum(raised, axis=1, keepdims=True)
        mass = jnp.dot(probs, weights, precision=lax.Precision.HIGHEST)
        blocks = lax.all_to_all(probs, "spot", split_axis=1, concat_axis=0, tiled=True)
        pred = lax.psum_scatter(
            jnp.dot(blocks, expr, precision=lax.Precision.HIGHEST),
            "spot",
            scatter_dimension=0,
            tiled=True,
        )
        gene_dot = jnp.sum(valid[:, None] * pred * target, axis=0)
        gene_pred = jnp.sum(valid[:, None] * pred * pred, axis=0)
        gene_true = jnp.sum(valid[:, None] * target * target, axis=0)
        mass_part = jnp.sum(valid * mass)
        kcell = valid * counted
        cell_part = jnp.sum(kcell)
        spot_dot = jnp.sum(pred * target, axis=1)
        spot_pred = jnp.sum(pred * pred, axis=1)
        spot_true = jnp.sum(target * target, axis=1)
        gene_dot, gene_pred, gene_true, mass_total, cell_total = lax.psum(
            (gene_dot, gene_pred, gene_true, mass_part, cell_part), "spot"
        )
        spot_dot, spot_pred, spot_true = lax.psum((spot_dot, spot_pred, spot_true), "gene")
        gene_inv = lax.rsqrt(gene_pred * gene_true + tiny)
        cos_gene = gene_dot * gene_inv
        spot_inv = lax.rsqrt(spot_pred * spot_true + tiny)
        cos_spot = spot_dot * spot_inv
        share = kcell / cell_total
        scale_count = slide_spots[slide].astype(jnp.float32)
        kl_part = jnp.sum(
            share * (jnp.log(counted) - jnp.log(cell_total) - jnp.log(mass) + jnp.log(mass_total))
        )
        loss_local = loss_local - gene_share * jnp.sum(cos_gene)
        loss_local = loss_local + row_share * (scale_count * kl_part - jnp.sum(valid * cos_spot))
        gene_back = cos_gene * gene_true / (gene_pred * gene_true + tiny)
        spot_back = cos_spot * spot_true / (spot_pred * spot_true + tiny)
        dpred = -valid[:, None] * (
            target * (gene_inv[None, :] + spot_inv[:, None])
            - pred * gene_back[None, :]
            - pred * spot_back[:, None]
        )
        dmass = scale_count * valid * (1.0 / mass_total - share / mass)
        pred_list.append(pred)
        grads_full, mass_full = (
            lax.all_gather(dpred, "spot", axis=0, tiled=True),
            lax.all_gather(dmass, "spot", axis=0, tiled=True),
        )
        dprob_cells = jnp.dot(grads_full, expr.T, precision=lax.Precision.HIGHEST)
        dprob_cells = lax.psum(dprob_cells, "gene")
        expr_acc = expr_acc + lax.dot_general(
            blocks, grads_full, (((0,), (0,)), ((), ())), precision=lax.Precision.HIGHEST
        )
        dprob_cells = dprob_cells + mass_full[:, None] * own_weights[None, :]
        dprob_rows = lax.all_to_all(dprob_cells, "spot", split_axis=0, concat_axis=1, tiled=True)
        inner = jnp.sum(probs * dprob_rows, axis=1, keepdims=True)
        dlogit = probs * (dprob_rows - inner)
        grad_list.append(dlogit)
    loss = lax.psum(loss_local, ("spot", "gene"))
    return (jnp.stack(pred_list), loss, jnp.stack(grad_list), expr_acc)


def solution(mesh):
    places = mesh.shape["spot"]

    def on_device(logits, expr, spatial, slide_spots, spot_cells, cell_prior):
        if places == PLANE * PLANE and mesh.shape["gene"] == 2 and expr.shape[1] == sum(FORWARD):
            return plane_call(
                logits, expr, spatial, slide_spots, spot_cells, cell_prior, places // PLANE
            )
        return general_plan(logits, expr, spatial, slide_spots, spot_cells, cell_prior)

    in_specs = (
        P(None, "spot", None),
        P("spot", "gene"),
        P(None, "spot", "gene"),
        P(),
        P(None, "spot"),
        P(),
    )
    out_specs = (P(None, "spot", "gene"), P(), P(None, "spot", None), P("spot", "gene"))
    return jax.shard_map(
        on_device, mesh=mesh, in_specs=in_specs, out_specs=out_specs, check_vma=False
    )
```

```python
import functools

import jax
import jax.numpy as jnp
from jax import lax
from jax.experimental import pallas as pl
from jax.experimental.pallas import tpu as pltpu
from jax.sharding import PartitionSpec as P

tiny = 1e-06
fixed_point = 16384.0
F32 = jnp.float32
BF16 = jnp.bfloat16
MESH = pl.DeviceIdType.MESH

PLANE = 4
LANES = 128
STEP_ROWS = 16
BLOCK = 32
TALL = 256
FORWARD = (128, 256, 256, 128, 128, 128)
BACKWARD = (128, 128, 128, 256, 384)
SPLIT = 2
LEAD = 1
NEAR_LEAD = 3
EARLY = 3
STEPS = (
    ("far", 0),
    ("far", 1),
    ("near", 0),
    ("share",),
    ("far", 2),
    ("far", 3),
    ("take",),
    ("whole", 0),
    ("near", 1),
    ("product", 0),
    ("sum", 0),
    ("whole", 1),
    ("near", 2),
    ("product", 1),
    ("whole", 2),
    ("product", 2),
    ("whole", 3),
    ("near", 3),
    ("product", 3),
    ("far", 4),
    ("whole", 4),
    ("near", 4),
    ("product", 4),
    ("sum", 1),
    ("turn", 0),
    ("far", 5),
    ("whole", 5),
    ("near", 5),
    ("product", 5),
    ("sum", 2),
    ("plane", 0),
    ("turn", 1),
    ("sum", 3),
    ("line", 0),
    ("sum", 4),
    ("sum", 5),
    ("plane", 1),
    ("cores",),
    ("genes", 0),
    ("spots",),
    ("grad", 0),
    ("grad", 1),
    ("grad", 2),
    ("line", 1),
    ("backward", 0),
    ("grad", 3),
    ("backward", 1),
    ("add_near", 0),
    ("genes", 1),
    ("backward", 2),
    ("probs", 0),
    ("probs", 1),
    ("grad", 4),
    ("add_far", 0),
    ("expr", 0),
    ("add_near", 1),
    ("probs", 2),
    ("terms",),
    ("backward", 3),
    ("probs", 3),
    ("add_near", 2),
    ("add_far", 1),
    ("backward", 4),
    ("probs", 4),
    ("exchange",),
    ("add_near", 3),
    ("add_far", 2),
    ("left",),
    ("return",),
    ("loss",),
    ("add_far", 3),
    ("expr", 1),
    ("add_near", 4),
    ("logits",),
    ("add_far", 4),
    ("expr", 2),
    ("expr", 3),
    ("expr", 4),
)


def halves(value):
    high = value.astype(BF16)
    return high, (value - high.astype(F32)).astype(BF16)


def threefold(value):
    high, low = halves(value)
    return jnp.concatenate([high, high, low], axis=1)


def product(a, b, contract):
    return lax.dot_general(a, b, (contract, ((), ())), preferred_element_type=F32)


def plane_kernel(lines, forward_widths, backward_widths, *refs):
    chunks, turns = len(forward_widths), len(backward_widths)
    (
        (logits_ref, expr_ref, spatial_ref, count_in, cells_in, prior_in),
        (pr, loss_ref, glog, ge),
        (count_ref, cells_ref, prior_ref, lg, lq, tg, ex, pq, ab, af, probs_3, turned_3, expr_3, sacc, s1, s2, gv, ss, rowv, rs),
        (grad_3, factor, t0, p0, vr, fs, fx, fy, fz, fr, inn, l1, l2),
        (loc, ou_s, ou_r, od_s, od_r, fu_s, fu_r, fd_s, fd_r, a_s, a_r, a2_s, a2_r, r_s, r_r),
        (c_s, c_r, s1_s, s1_r, s2_s, s2_r, ss_s, ss_r, d_s, d_r, ru_s, ru_r, rd_s, rd_r),
        (f_s, f_r, fx_s, fx_r, go_s, go_r, in_s, in_r, l1_s, l1_r, l2_s, l2_r, t0_s, t0_r, p0_s, p0_r, vr_s, vr_r),
        bb,
        cs,
        cr,
        ds,
        es,
        ru,
        rd,
    ) = grouped(refs, (6, 4, 20, 13, 15, 14, 18, chunks, chunks, chunks, turns, turns, turns, turns))
    place = lax.axis_index("spot")
    core = lax.axis_index("gene")
    z = place // PLANE
    q = place % PLANE
    col, row = q % 2, q // 2
    mates = ((1 - row) * 2 + 1 - col, row * 2 + 1 - col, (1 - row) * 2 + col)
    others = tuple((z + step) % lines for step in range(1, lines))
    up, down = (place + PLANE, core), (place - PLANE, core)
    sibling = (place, 1 - core)
    slides, slide_rows = logits_ref.shape[0], logits_ref.shape[1]
    rows = slides * slide_rows
    cb = expr_ref.shape[0]
    genes = expr_ref.shape[1]
    last = lines - 1

    def mate(p):
        return (z * PLANE + p, core)

    def send(src, dst, send_sem, recv_sem, device):
        copy = pltpu.make_async_remote_copy(
            src_ref=src, dst_ref=dst, send_sem=send_sem, recv_sem=recv_sem, device_id=device, device_id_type=MESH
        )
        copy.start()

    def arrived(dst, recv_sem):
        pltpu.make_async_copy(dst, dst, recv_sem).wait()

    sent = arrived

    def cols(k):
        return pl.ds(sum(forward_widths[:k]), forward_widths[k])

    def turn_cols(k):
        return pl.ds(sum(backward_widths[:k]), backward_widths[k])

    def block(index):
        return pl.ds(pl.multiple_of(index * cb, cb), cb)

    def share(index):
        return pl.ds(pl.multiple_of(index * rows, rows), rows)

    def half(index):
        return pl.ds(pl.multiple_of(index * slide_rows, slide_rows), slide_rows)

    small = ((prior_in, prior_ref), (count_in, count_ref), (cells_in, cells_ref))
    pltpu.make_async_copy(expr_ref, ex, loc.at[2 * slides]).start()
    for m in range(slides):
        pltpu.make_async_copy(logits_ref.at[m], lg.at[half(m)], loc.at[m]).start()
    for at, (src, dst) in enumerate(small):
        pltpu.make_async_copy(src, dst, loc.at[2 * slides + 1 + at]).start()
    for m in range(slides):
        pltpu.make_async_copy(spatial_ref.at[m], tg.at[half(m)], loc.at[slides + m]).start()

    barrier = pltpu.get_barrier_semaphore()
    for p in mates:
        pl.semaphore_signal(barrier, inc=1, device_id=mate(p), device_id_type=MESH)
    for o in others:
        pl.semaphore_signal(barrier, inc=1, device_id=(o * PLANE + q, core), device_id_type=MESH)
    pl.semaphore_signal(barrier, inc=1, device_id=sibling, device_id_type=MESH)
    pltpu.make_async_copy(expr_ref, ex, loc.at[2 * slides]).wait()
    for k in range(chunks):
        bb[k][block(z), :] = ex[:, cols(k)]
    for m in range(slides):
        pltpu.make_async_copy(logits_ref.at[m], lg.at[half(m)], loc.at[m]).wait()
    for p in range(PLANE):
        for line in range(lines):
            lq[p, :, pl.ds(line * cb, cb)] = lg[half(core), pl.ds((line * PLANE + p) * cb, cb)]
    pl.semaphore_wait(barrier, len(mates) + len(others) + 1)

    def own_up(k):
        here = bb[k].at[block(z)]
        send(here, here, ou_s.at[k], ou_r.at[k], up)

    def own_down(k):
        here = bb[k].at[block(z)]
        send(here, here, od_s.at[k], od_r.at[k], down)

    def low(at):
        return 2 * at < lines

    for at in range(lines):

        @pl.when(z == at)
        def _():
            for k in range(chunks):
                if at < last and (at == 0 or k < (LEAD if low(at) else NEAR_LEAD)):
                    own_up(k)
                if at > 0 and (at == last or k < (NEAR_LEAD if low(at) else LEAD)):
                    own_down(k)

    for p in mates:
        send(lq.at[p], ab.at[q, half(core)], a_s, a_r.at[q], mate(p))

    def from_below(k, at):
        arrived(bb[k].at[pl.ds((at - 1) * cb, cb)], ou_r.at[k])
        if at > 1:
            arrived(bb[k].at[pl.ds(0, (at - 1) * cb)], fu_r.at[k])

    def from_above(k, at):
        arrived(bb[k].at[pl.ds((at + 1) * cb, cb)], od_r.at[k])
        if at < last - 1:
            arrived(bb[k].at[pl.ds((at + 2) * cb, (last - 1 - at) * cb)], fd_r.at[k])

    def upward(k, at):
        from_below(k, at)
        here = bb[k].at[pl.ds(0, at * cb)]
        send(here, here, fu_s.at[k], fu_r.at[k], up)

    def downward(k, at):
        from_above(k, at)
        here = bb[k].at[pl.ds((at + 1) * cb, (last - at) * cb)]
        send(here, here, fd_s.at[k], fd_r.at[k], down)

    def forward_far(k):
        for at in range(1, last):

            @pl.when(z == at)
            def _():
                (upward if low(at) else downward)(k, at)
                if k + LEAD < chunks:
                    (own_up if low(at) else own_down)(k + LEAD)

    def forward_near(k):
        for at in range(1, last):

            @pl.when(z == at)
            def _():
                (downward if low(at) else upward)(k, at)
                if k + NEAR_LEAD < chunks:
                    (own_down if low(at) else own_up)(k + NEAR_LEAD)

    def gathered(k):
        @pl.when(z == 0)
        def _():
            from_above(k, 0)

        @pl.when(z == last)
        def _():
            from_below(k, last)

    for at, (src, dst) in enumerate(small):
        pltpu.make_async_copy(src, dst, loc.at[2 * slides + 1 + at]).wait()
    weights = prior_ref[...].astype(F32) / fixed_point

    @pl.loop(0, rows // STEP_ROWS)
    def _(step):
        at = pl.ds(pl.multiple_of(step * STEP_ROWS, STEP_ROWS), STEP_ROWS)
        value = lg[at, :]
        peak = jnp.max(value, axis=1, keepdims=True)
        raised = jnp.exp(value - peak)
        scale = 1.0 / jnp.sum(raised, axis=1, keepdims=True)
        probs = raised * scale
        mass_rows = jnp.sum(probs * weights, axis=1, keepdims=True)
        rowv[0, at, :] = jnp.broadcast_to(mass_rows, (STEP_ROWS, LANES))
        rowv[1, at, :] = jnp.broadcast_to(peak, (STEP_ROWS, LANES))
        rowv[2, at, :] = jnp.broadcast_to(scale, (STEP_ROWS, LANES))
        for p in range(PLANE):
            for line in range(lines):
                at_cells = (line * PLANE + p) * cb
                pq[p, at, pl.ds(line * cb, cb)] = probs[:, at_cells : at_cells + cb]

    wide = lax.broadcasted_iota(jnp.int32, (rows, LANES), 1)
    rs[q] = jnp.where(wide == 0, rowv[1], rowv[2]).T[0:8]
    for p in mates:
        send(rs.at[q], rs.at[q], r_s, r_r.at[q], mate(p))

    rid = lax.broadcasted_iota(jnp.int32, (rows, 1), 0)
    first = rid < slide_rows
    position = place * slide_rows + jnp.where(first, rid, rid - slide_rows)
    count = jnp.where(first, count_ref[0], count_ref[1])
    valid = (position < count).astype(F32)
    scale_count = count.astype(F32)
    square = (slide_rows, slide_rows)
    eye = lax.broadcasted_iota(jnp.int32, square, 0) == lax.broadcasted_iota(jnp.int32, square, 1)
    counted = jnp.concatenate(
        [
            jnp.sum(jnp.where(eye, cells_ref[m : m + 1, :].astype(F32), 0.0), axis=1, keepdims=True)
            for m in range(slides)
        ],
        axis=0,
    )
    mass = rowv[0, :, 0:1]
    kcell = valid * counted

    def by_slide(value):
        return [jnp.sum(value[m * slide_rows : (m + 1) * slide_rows], axis=0, keepdims=True) for m in range(slides)]

    mass_parts = by_slide(valid * mass)
    cell_parts = by_slide(kcell)
    lane = lax.broadcasted_iota(jnp.int32, (1, LANES), 1)
    scalars = jnp.zeros((1, LANES), F32)
    for at, value in enumerate(mass_parts + cell_parts):
        scalars = jnp.where(lane == at, value, scalars)
    for m in range(slides):
        pltpu.make_async_copy(spatial_ref.at[m], tg.at[half(m)], loc.at[slides + m]).wait()

    head = backward_widths[0]
    t0[q] = tg[:, 0:head]
    for p in mates:
        send(t0.at[q], t0.at[q], t0_s, t0_r.at[q], mate(p))
    sacc[...] = jnp.zeros_like(sacc)
    s1[q, 3 * slides :, :] = jnp.zeros((8 - 3 * slides, genes), F32)
    s1[q, 3 * slides : 3 * slides + 1, 0:LANES] = scalars

    def share_logits():
        for p in (mates[1], mates[2], mates[0]):
            here = ab.at[p, half(core)]
            arrived(here, a_r.at[p])
            send(here, here, a2_s, a2_r.at[p], sibling)

    def lay_probs(p, at, value):
        af[p, at, :] = value
        there = pl.ds(pl.multiple_of(p * rows + at.start, BLOCK), BLOCK)
        probs_3[there, :] = threefold(value)

    def take_probs():
        in_blocks(0, rows, lambda at: lay_probs(q, at, pq[q, at, :]))
        for p in (mates[1], mates[2], mates[0]):
            arrived(rs.at[p], r_r.at[p])
            arrived(ab.at[p, half(1 - core)], a2_r.at[p])
            rowv[1] = jnp.concatenate([rs[p].T, jnp.zeros((rows, LANES - 8), F32)], axis=1)

            def take(at):
                probs = jnp.exp(ab[p, at, :] - rowv[1, at, 0:1]) * rowv[1, at, 1:2]
                lay_probs(p, at, probs)

            in_blocks(0, rows, take)

    def transpose(part):
        @pl.loop(0, PLANE // 2)
        def _(step):
            p = part * (PLANE // 2) + step
            high, low_part = halves(af[p].T)
            for third, value in enumerate((high, high, low_part)):
                turned_3[:, pl.ds(pl.multiple_of(third * PLANE * rows + p * rows, rows), rows)] = value

    def in_blocks(start, count, body):
        @pl.loop(0, count // BLOCK)
        def _(step):
            body(pl.ds(pl.multiple_of(start + step * BLOCK, BLOCK), BLOCK))

    quarter = lines * cb

    def lay_factor(at, length, width, value):
        high, low_part = halves(value)
        for third, part in enumerate((high, low_part, high)):
            here = pl.ds(pl.multiple_of(third * length + at.start, BLOCK), BLOCK)
            factor[here, 0:width] = part

    def keep_expr(k, at, value):
        start = sum(forward_widths[:k])
        for turn in range(turns):
            origin, width = sum(backward_widths[:turn]), backward_widths[turn]
            lo, hi = max(start, origin), min(start + forward_widths[k], origin + width)
            if lo < hi:
                high, low_part = halves(value[:, lo - start : hi - start])
                for third, part in enumerate((high, low_part, high)):
                    expr_3[at, pl.ds(3 * origin + third * width + lo - origin, hi - lo)] = part

    def three_turn_cols(k):
        return pl.ds(3 * sum(backward_widths[:k]), 3 * backward_widths[k])

    def forward_product(k):
        width = forward_widths[k]

        def lay(at):
            value = bb[k][at, :]
            lay_factor(at, quarter, width, value)
            keep_expr(k, at, value)

        in_blocks(0, quarter, lay)
        if k < chunks - 1:

            @pl.loop(0, PLANE * rows // TALL)
            def _(step):
                tall = pl.ds(pl.multiple_of(step * TALL, TALL), TALL)
                cs[k][tall, :] = product(probs_3[tall, :], factor[0 : 3 * quarter, 0:width], ((1,), (0,)))

            for p in mates:
                pass_pred(k, p)
        else:
            for side, served in ((1 - row, (mates[0], mates[2])), (row, (mates[1],))):
                pair = pl.ds(pl.multiple_of(2 * side * rows, 2 * rows), 2 * rows)
                cs[k][pair, :] = product(probs_3[pair, :], factor[0 : 3 * quarter, 0:width], ((1,), (0,)))
                for p in served:
                    pass_pred(k, p)

    def pass_pred(k, p):
        send(cs[k].at[share(p)], cr[k].at[q], c_s.at[k], c_r.at[k, q], mate(p))

    def finish_pred(k):
        total = cs[k][share(q), :]
        for p in mates:
            arrived(cr[k].at[p], c_r.at[k, p])
            total = total + cr[k][p]
        pr[:, cols(k)] = total
        if k == 0:
            p0[q] = total[:, 0:head]
            for p in mates:
                send(p0.at[q], p0.at[q], p0_s, p0_r.at[q], mate(p))
        truth = tg[:, cols(k)]
        for at, value in enumerate((total * truth, total * total, truth * truth)):
            sacc[at] += lane_groups(value)
        kept = valid * total
        stats = by_slide(kept * truth) + by_slide(kept * total) + by_slide(valid * truth * truth)
        s1[q, 0 : 3 * slides, cols(k)] = jnp.concatenate(stats, axis=0)

    early = sum(forward_widths[:EARLY])
    parts = (pl.ds(0, early), pl.ds(early, genes - early))

    def sum_plane(at):
        for p in mates:
            send(s1.at[q, :, parts[at]], s1.at[q, :, parts[at]], s1_s, s1_r.at[at, q], mate(p))

    def sum_line(at):
        for p in mates:
            arrived(s1.at[p, :, parts[at]], s1_r.at[at, p])
        s2[z, :, parts[at]] = (s1[0, :, parts[at]] + s1[1, :, parts[at]]) + (s1[2, :, parts[at]] + s1[3, :, parts[at]])
        for o in others:
            send(s2.at[z, :, parts[at]], s2.at[z, :, parts[at]], s2_s, s2_r.at[at, z], (o * PLANE + q, core))

    kept = {}

    def finish_genes(at):
        for o in others:
            arrived(s2.at[o, :, parts[at]], s2_r.at[at, o])
        total = s2[0, :, parts[at]]
        for line in range(1, lines):
            total = total + s2[line, :, parts[at]]
        gene_dot, gene_pred, gene_true = total[0:2], total[2:4], total[4:6]
        gene_inv = lax.rsqrt(gene_pred * gene_true + tiny)
        cos_gene = gene_dot * gene_inv
        gv[0:2, parts[at]] = gene_inv
        gv[2:4, parts[at]] = cos_gene * gene_true / (gene_pred * gene_true + tiny)
        kept["genes", at] = jnp.sum(jnp.sum(cos_gene, axis=1, keepdims=True), axis=0, keepdims=True)
        if at == 0:
            kept["mass"] = jnp.where(first, total[6:7, 0:1], total[6:7, 1:2])
            kept["cells"] = jnp.where(first, total[6:7, 2:3], total[6:7, 3:4])

    def sum_cores():
        sums = [jnp.sum(sacc[at], axis=1, keepdims=True) for at in range(3)]
        ss[core] = jnp.where(wide == 0, sums[0], jnp.where(wide == 1, sums[1], sums[2])).T[0:8]
        send(ss.at[core], ss.at[core], ss_s, ss_r, sibling)

    def finish_spots():
        lane_id = lax.broadcasted_iota(jnp.int32, (1, rows), 1)
        first_lane = lane_id < slide_rows
        lane_position = place * slide_rows + jnp.where(first_lane, lane_id, lane_id - slide_rows)
        lane_valid = (lane_position < jnp.where(first_lane, count_ref[0], count_ref[1])).astype(F32)
        arrived(ss.at[1 - core], ss_r)
        spot = ss[0] + ss[1]
        spot_dot, spot_pred, spot_true = spot[0:1], spot[1:2], spot[2:3]
        spot_inv = lax.rsqrt(spot_pred * spot_true + tiny)
        cos_spot = spot_dot * spot_inv
        spot_back = cos_spot * spot_true / (spot_pred * spot_true + tiny)
        kept["cos"] = jnp.sum(lane_valid * cos_spot, axis=1, keepdims=True)
        vectors = [lane_valid * spot_inv, lane_valid * spot_back, lane_valid, jnp.zeros((5, rows), F32)]
        vr[q] = jnp.concatenate(vectors, axis=0)
        sacc[0] = jnp.zeros_like(sacc[0])

    def gradient(truth, guess, by_row, k):
        pieces = []
        for m in range(slides):
            lo, hi = m * slide_rows, (m + 1) * slide_rows
            inverse, back = gv[m : m + 1, turn_cols(k)], gv[2 + m : 3 + m, turn_cols(k)]
            spot_inv, spot_back, spot_valid = by_row[lo:hi, 0:1], by_row[lo:hi, 1:2], by_row[lo:hi, 2:3]
            pieces.append(
                guess[lo:hi] * (spot_valid * back + spot_back) - truth[lo:hi] * (spot_valid * inverse + spot_inv)
            )
        return jnp.concatenate(pieces, axis=0)

    def head_gradient():
        for p in mates:
            arrived(t0.at[p], t0_r.at[p])
            arrived(p0.at[p], p0_r.at[p])
            arrived(vr.at[p], vr_r.at[p])
        for p in range(PLANE):
            ds[0][share(p), :] = gradient(t0[p], p0[p], vr[p].T, 0)
        sacc[0] += lane_groups(ds[0][share(q), :] * p0[q])

    def send_grad(k):
        if k == 0:
            for p in mates:
                send(vr.at[q], vr.at[q], vr_s, vr_r.at[q], mate(p))
            kept["by_row"] = vr[q].T
            return
        grad = gradient(tg[:, turn_cols(k)], pr[:, turn_cols(k)], kept["by_row"], k)
        here = ds[k].at[share(q)]
        here[...] = grad
        for p in mates:
            send(here, here, d_s.at[k], d_r.at[k, q], mate(p))
        sacc[0] += lane_groups(grad * pr[:, turn_cols(k)])

    def send_terms():
        mass_total, cell_total = kept["mass"], kept["cells"]
        portion = kcell / cell_total
        kl_rows = portion * (jnp.log(counted) - jnp.log(cell_total) - jnp.log(mass) + jnp.log(mass_total))
        dmass = scale_count * valid * (1.0 / mass_total - portion / mass)
        terms = jnp.sum(scale_count * kl_rows, axis=0, keepdims=True) - kept["cos"]
        l1[q] = jnp.broadcast_to(terms, (8, LANES))
        for p in mates:
            send(l1.at[q], l1.at[q], l1_s, l1_r.at[q], mate(p))
        inner = jnp.sum(sacc[0], axis=1, keepdims=True)
        inn[core] = jnp.where(wide == 0, inner, kept["genes", 0] + kept["genes", 1])
        send(inn.at[core], inn.at[core], in_s, in_r, sibling)
        rowv[1] = jnp.broadcast_to(dmass, (rows, LANES))

    middle = lines // 2

    def backward_product(k):
        if k == 0:
            head_gradient()
        else:
            for p in mates:
                arrived(ds[k].at[share(p)], d_r.at[k, p])
        width, spots = backward_widths[k], PLANE * rows

        def lay(at):
            value = ds[k][at, :]
            lay_factor(at, spots, width, value)
            grad_3[at, three_turn_cols(k)] = threefold(value)

        in_blocks(0, spots, lay)
        if not halved(k):

            @pl.loop(0, quarter // TALL)
            def _(step):
                tall = pl.ds(pl.multiple_of(step * TALL, TALL), TALL)
                es[k][tall, :] = product(turned_3[tall, :], factor[0 : 3 * spots, 0:width], ((1,), (0,)))

        for turn in range(2):
            if halved(k):
                side = (1 - z // middle) if turn == 0 else z // middle
                pair = pl.ds(pl.multiple_of(side * middle * cb, middle * cb), middle * cb)
                es[k][pair, :] = product(turned_3[pair, :], factor[0 : 3 * spots, 0:width], ((1,), (0,)))

            @pl.when(z == 0)
            def _():
                if halved(k):
                    pass_up(k, middle if turn == 0 else 1, middle if turn == 0 else middle - 1, turn)
                elif whole(k):
                    if turn == 0:
                        pass_up(k, 1, last, 0)
                elif turn == 0:
                    for line in range(last, 0, -1):
                        pass_up(k, line, 1, line)

            @pl.when(z == last)
            def _():
                if halved(k):
                    pass_down(k, 0 if turn == 0 else middle, middle if turn == 0 else middle - 1, turn)
                elif whole(k):
                    if turn == 0:
                        pass_down(k, 0, last, 0)
                elif turn == 0:
                    for line in range(last):
                        pass_down(k, line, 1, line)

    def halved(k):
        return k == 0

    def whole(k):
        return 0 < k < turns - SPLIT

    def pass_up(k, line, count, slot):
        here = pl.ds(line * cb, count * cb)
        send(es[k].at[here], ru[k].at[here], ru_s.at[k], ru_r.at[k, slot], up)

    def pass_down(k, line, count, slot):
        here = pl.ds(line * cb, count * cb)
        send(es[k].at[here], rd[k].at[here], rd_s.at[k], rd_r.at[k, slot], down)

    def take_up(k, line, count, slot):
        arrived(ru[k].at[pl.ds(line * cb, count * cb)], ru_r.at[k, slot])

    def take_down(k, line, count, slot):
        arrived(rd[k].at[pl.ds(line * cb, count * cb)], rd_r.at[k, slot])

    def add_up(k, line, count):
        def add(at):
            es[k][at, :] += ru[k][at, :]

        in_blocks(line * cb, count * cb, add)

    def add_down(k, line, count):
        def add(at):
            es[k][at, :] += rd[k][at, :]

        in_blocks(line * cb, count * cb, add)

    def rising(k, at):
        if halved(k) or whole(k):
            start = middle if halved(k) else at
            take_up(k, start, lines - start, 0)
            above = max(at + 1, start)
            add_up(k, above, lines - above)
            pass_up(k, above, lines - above, 0)
        else:
            for line in range(last, at, -1):
                take_up(k, line, 1, line)
                add_up(k, line, 1)
                pass_up(k, line, 1, line)

    def falling(k, at):
        if halved(k) or whole(k):
            end = middle if halved(k) else at + 1
            take_down(k, 0, end, 0)
            below = min(at, end)
            add_down(k, 0, below)
            pass_down(k, 0, below, 0)
        else:
            for line in range(at):
                take_down(k, line, 1, line)
                add_down(k, line, 1)
                pass_down(k, line, 1, line)

    def add_near(k):
        for at in range(1, last):

            @pl.when(z == at)
            def _():
                (rising if low(at) else falling)(k, at)

    def add_far(k):
        for at in range(1, last):

            @pl.when(z == at)
            def _():
                (falling if low(at) else rising)(k, at)

    def finish_expr(k):
        for at in range(lines):

            @pl.when(z == at)
            def _():
                if at > 0:
                    if halved(k) and at < middle:
                        take_up(k, at, 1, 1)
                    elif at == last and (halved(k) or whole(k)):
                        take_up(k, at, 1, 0)
                    elif not halved(k) and not whole(k):
                        take_up(k, at, 1, at)
                if at < last:
                    if halved(k) and at >= middle:
                        take_down(k, at, 1, 1)
                    elif at == 0 and (halved(k) or whole(k)):
                        take_down(k, at, 1, 0)
                    elif not halved(k) and not whole(k):
                        take_down(k, at, 1, at)

        from_low, from_high = z > 0, z < last

        @pl.loop(0, cb // BLOCK)
        def _(step):
            here = pl.ds(pl.multiple_of(step * BLOCK, BLOCK), BLOCK)
            own = pl.ds(pl.multiple_of(z * cb + step * BLOCK, BLOCK), BLOCK)
            total = es[k][own, :]
            total = total + jnp.where(from_low, ru[k][own, :], 0.0)
            ge[here, turn_cols(k)] = total + jnp.where(from_high, rd[k][own, :], 0.0)

    def probs_gradient(k):
        at = three_turn_cols(k)

        @pl.loop(0, PLANE * rows // TALL)
        def _(step):
            tall = pl.ds(pl.multiple_of(step * TALL, TALL), TALL)
            part = product(grad_3[tall, at], expr_3[:, at], ((1,), (1,)))
            if k == 0:
                fs[tall, :] = part
            else:
                fs[tall, :] += part

    def slide_of(p, m):
        return pl.ds(pl.multiple_of(p * rows + m * slide_rows, slide_rows), slide_rows)

    def sum_probs_cores():
        for p in mates + (q,):
            fx[p] = fs[slide_of(p, 1 - core), :]
            send(fx.at[p], fy.at[p], fx_s, fx_r.at[p], sibling)

    def return_probs():
        for p in mates:
            arrived(fy.at[p], fx_r.at[p])
            fz[p] = fs[slide_of(p, core), :] + fy[p]
            send(fz.at[p], fr.at[q], f_s, f_r.at[q], mate(p))
        arrived(fy.at[q], fx_r.at[q])
        fr[q] = fs[slide_of(q, core), :] + fy[q]

    def pass_terms():
        for p in mates:
            arrived(l1.at[p], l1_r.at[p])
        l2[z] = (l1[0] + l1[1]) + (l1[2] + l1[3])
        for o in others:
            send(l2.at[z], l2.at[z], l2_s, l2_r.at[z], (o * PLANE + q, core))

    def part_of(slide, m):
        start = slide * slide_rows + m * (slide_rows // 2)
        return pl.ds(pl.multiple_of(start, slide_rows // 2), slide_rows // 2)

    def finish_logits():
        arrived(inn.at[1 - core], in_r)
        rowv[2] = (inn[0] + inn[1]) + rowv[1] * rowv[0]
        for p in mates:
            arrived(fr.at[p], f_r.at[p])
        for m in range(2):

            @pl.loop(0, slide_rows // STEP_ROWS // 2)
            def _(step):
                row_at = (m * (slide_rows // STEP_ROWS // 2) + step) * STEP_ROWS
                at = pl.ds(pl.multiple_of(row_at, STEP_ROWS), STEP_ROWS)
                whole_at = pl.ds(pl.multiple_of(core * slide_rows + row_at, STEP_ROWS), STEP_ROWS)
                by_mass, total_inner = rowv[1, whole_at, 0:1], rowv[2, whole_at, 0:1]
                for p in range(PLANE):
                    for line in range(lines):
                        here, there = pl.ds(line * cb, cb), (line * PLANE + p) * cb
                        grad = fr[p, at, here] + by_mass * weights[:, there : there + cb]
                        glog[whole_at, pl.ds(there, cb)] = pq[p, whole_at, here] * (grad - total_inner)

            here = part_of(core, m)
            send(glog.at[here], glog.at[here], go_s, go_r.at[m], sibling)

    def forward_left():
        for k in range(chunks):

            @pl.when(z < last)
            def _():
                sent(bb[k].at[block(z)], ou_s.at[k])

            @pl.when(z > 0)
            def _():
                sent(bb[k].at[block(z)], od_s.at[k])

            for at in range(1, last):

                @pl.when(z == at)
                def _():
                    sent(bb[k].at[pl.ds(0, at * cb)], fu_s.at[k])
                    sent(bb[k].at[pl.ds((at + 1) * cb, (last - at) * cb)], fd_s.at[k])

        three = pl.ds(0, len(mates))
        sent(ab.at[three, half(0)], a_s)
        sent(ab.at[three, half(0)], a2_s)
        sent(rs.at[three], r_s)
        sent(t0.at[three], t0_s)
        sent(p0.at[three], p0_s)
        for k in range(chunks):
            sent(cr[k].at[three], c_s.at[k])
        sent(s1.at[three], s1_s)
        sent(s2.at[pl.ds(0, last)], s2_s)
        sent(ss.at[0], ss_s)

    steps = {
        "far": forward_far,
        "near": forward_near,
        "share": share_logits,
        "take": take_probs,
        "whole": gathered,
        "product": forward_product,
        "sum": finish_pred,
        "turn": transpose,
        "plane": sum_plane,
        "line": sum_line,
        "genes": finish_genes,
        "cores": sum_cores,
        "spots": finish_spots,
        "grad": send_grad,
        "terms": send_terms,
        "backward": backward_product,
        "probs": probs_gradient,
        "exchange": sum_probs_cores,
        "return": return_probs,
        "loss": pass_terms,
        "logits": finish_logits,
        "add_near": add_near,
        "add_far": add_far,
        "expr": finish_expr,
        "left": forward_left,
    }
    for name, *where in STEPS:
        steps[name](*where)

    for o in others:
        arrived(l2.at[o], l2_r.at[o])
    loss = l2[0]
    for line in range(1, lines):
        loss = loss + l2[line]
    loss_ref[...] = loss[0:1, 0:1] - (inn[0, 0:1, 1:2] + inn[1, 0:1, 1:2])
    for m in range(2):
        arrived(glog.at[part_of(1 - core, m)], go_r.at[m])

    for k in range(turns):
        for at in range(lines):

            @pl.when(z == at)
            def _():
                if at < last:
                    sent(es[k].at[pl.ds((at + 1) * cb, (last - at) * cb)], ru_s.at[k])
                if at > 0:
                    sent(es[k].at[pl.ds(0, at * cb)], rd_s.at[k])

    three = pl.ds(0, len(mates))
    for k in range(1, turns):
        sent(ds[k].at[pl.ds(0, len(mates) * rows)], d_s.at[k])
    sent(vr.at[three], vr_s)
    sent(inn.at[0], in_s)
    sent(l1.at[three], l1_s)
    sent(l2.at[pl.ds(0, last)], l2_s)
    sent(fr.at[three], f_s)
    sent(fx, fx_s)
    sent(glog.at[half(0)], go_s)


def lane_groups(value):
    parts = [value[:, at : at + LANES] for at in range(0, value.shape[1], LANES)]
    return functools.reduce(lambda a, b: a + b, parts)


def grouped(refs, sizes):
    at = 0
    for size in sizes:
        yield refs[at : at + size]
        at += size


def deliver(pred_in, loss_in, glog_in, gexp_in, pred_ref, loss_ref, glog_ref, gexp_ref, sems):
    slides, slide_rows = pred_ref.shape[0], pred_ref.shape[1]
    pairs = [(gexp_in, gexp_ref), (loss_in, loss_ref)]
    for m in range(slides):
        part = pl.ds(m * slide_rows, slide_rows)
        pairs += [(glog_in.at[part], glog_ref.at[m]), (pred_in.at[part], pred_ref.at[m])]
    copies = [pltpu.make_async_copy(src, dst, sems.at[at]) for at, (src, dst) in enumerate(pairs)]
    for copy in copies:
        copy.start()
    for copy in copies:
        copy.wait()


def plane_call(logits, expr, spatial, slide_spots, spot_cells, cell_prior, lines):
    slides, slide_rows, cells = logits.shape
    rows = slides * slide_rows
    cb, genes = expr.shape
    quarter = lines * cb
    spots = PLANE * rows
    chunks, turns = len(FORWARD), len(BACKWARD)
    dma = pltpu.SemaphoreType.DMA
    vmem = pltpu.VMEM
    anywhere = pl.BlockSpec(memory_space=pl.ANY)
    in_vmem = pl.BlockSpec(memory_space=pltpu.VMEM)
    scratch = [
        pltpu.SMEM((slides,), jnp.int32),
        vmem((slides, slide_rows), jnp.int32),
        vmem((1, cells), jnp.int32),
        vmem((rows, cells), F32),
        vmem((PLANE, slide_rows, quarter), F32),
        vmem((rows, genes), F32),
        vmem((cb, genes), F32),
        vmem((PLANE, rows, quarter), F32),
        vmem((PLANE, rows, quarter), F32),
        vmem((PLANE, rows, quarter), F32),
        vmem((spots, 3 * quarter), BF16),
        vmem((quarter, 3 * spots), BF16),
        vmem((quarter, 3 * genes), BF16),
        vmem((3, rows, LANES), F32),
        vmem((PLANE, 8, genes), F32),
        vmem((lines, 8, genes), F32),
        vmem((8, genes), F32),
        vmem((2, 8, rows), F32),
        vmem((3, rows, LANES), F32),
        vmem((PLANE, 8, rows), F32),
        vmem((spots, 3 * genes), BF16),
        vmem((3 * max(quarter, spots), max(FORWARD + BACKWARD)), BF16),
        vmem((PLANE, rows, BACKWARD[0]), F32),
        vmem((PLANE, rows, BACKWARD[0]), F32),
        vmem((PLANE, 8, rows), F32),
        vmem((spots, quarter), F32),
        vmem((PLANE, slide_rows, quarter), F32),
        vmem((PLANE, slide_rows, quarter), F32),
        vmem((PLANE, slide_rows, quarter), F32),
        vmem((PLANE, slide_rows, quarter), F32),
        vmem((2, rows, LANES), F32),
        vmem((PLANE, 8, LANES), F32),
        vmem((lines, 8, LANES), F32),
        dma((2 * slides + 4,)),
        dma((chunks,)),
        dma((chunks,)),
        dma((chunks,)),
        dma((chunks,)),
        dma((chunks,)),
        dma((chunks,)),
        dma((chunks,)),
        dma((chunks,)),
        dma,
        dma((PLANE,)),
        dma,
        dma((PLANE,)),
        dma,
        dma((PLANE,)),
        dma((chunks,)),
        dma((chunks, PLANE)),
        dma,
        dma((2, PLANE)),
        dma,
        dma((2, lines)),
        dma,
        dma,
        dma((turns,)),
        dma((turns, PLANE)),
        dma((turns,)),
        dma((turns, lines)),
        dma((turns,)),
        dma((turns, lines)),
        dma,
        dma((PLANE,)),
        dma,
        dma((PLANE,)),
        dma,
        dma((2,)),
        dma,
        dma,
        dma,
        dma((PLANE,)),
        dma,
        dma((lines,)),
        dma,
        dma((PLANE,)),
        dma,
        dma((PLANE,)),
        dma,
        dma((PLANE,)),
    ]
    for shape, widths in (
        ((quarter,), FORWARD),
        ((spots,), FORWARD),
        ((PLANE, rows), FORWARD),
        ((spots,), BACKWARD),
        ((quarter,), BACKWARD),
        ((quarter,), BACKWARD),
        ((quarter,), BACKWARD),
    ):
        scratch += [vmem(shape + (width,), F32) for width in widths]
    in_hbm = functools.partial(pltpu.with_memory_space_constraint, memory_space=pltpu.HBM)
    in_place = functools.partial(pltpu.with_memory_space_constraint, memory_space=pltpu.VMEM)
    results = pl.pallas_call(
        functools.partial(plane_kernel, lines, FORWARD, BACKWARD),
        out_shape=(
            vmem((rows, genes), F32),
            vmem((1, 1), F32),
            vmem((rows, cells), F32),
            vmem((cb, genes), F32),
        ),
        in_specs=[anywhere] * 6,
        out_specs=(in_vmem,) * 4,
        scratch_shapes=scratch,
        compiler_params=pltpu.CompilerParams(
            collective_id=0, has_side_effects=True, vmem_limit_bytes=48 * 1024 * 1024
        ),
    )(*map(in_hbm, (logits, expr, spatial, slide_spots, spot_cells, cell_prior.reshape(1, cells))))
    pred, loss, grad_logits, grad_expr = pl.pallas_call(
        deliver,
        out_shape=(
            jax.ShapeDtypeStruct((slides, slide_rows, genes), F32),
            jax.ShapeDtypeStruct((1, 1), F32),
            jax.ShapeDtypeStruct((slides, slide_rows, cells), F32),
            jax.ShapeDtypeStruct((cb, genes), F32),
        ),
        in_specs=[anywhere] * 4,
        out_specs=(anywhere,) * 4,
        scratch_shapes=[dma((2 * slides + 2,))],
        compiler_params=pltpu.CompilerParams(vmem_limit_bytes=4 * 1024 * 1024),
    )(*map(in_place, results))
    return pred, loss.reshape(()), grad_logits, grad_expr


def general_plan(logits, expr, spatial, slide_spots, spot_cells, cell_prior):
    place = lax.axis_index("spot")
    side = lax.axis_index("gene")
    rows_all = logits.shape[1]
    cell_rows = expr.shape[0]
    weights = cell_prior.astype(jnp.float32) / fixed_point
    gene_share = (place == 0).astype(jnp.float32)
    row_share = (side == 0).astype(jnp.float32)
    own_weights = lax.dynamic_slice_in_dim(weights, place * cell_rows, cell_rows, 0)
    expr_acc = jnp.zeros((cell_rows, expr.shape[1]), jnp.float32)
    loss_local = jnp.zeros((), jnp.float32)
    pred_list = []
    grad_list = []
    for slide in range(logits.shape[0]):
        logit_rows = logits[slide]
        counted = spot_cells[slide].astype(jnp.float32)
        target = spatial[slide]
        positions = place * rows_all + jnp.arange(rows_all, dtype=jnp.int32)
        valid = (positions < slide_spots[slide]).astype(jnp.float32)
        peak = jnp.max(logit_rows, axis=1, keepdims=True)
        raised = jnp.exp(logit_rows - peak)
        probs = raised / jnp.sum(raised, axis=1, keepdims=True)
        mass = jnp.dot(probs, weights, precision=lax.Precision.HIGHEST)
        blocks = lax.all_to_all(probs, "spot", split_axis=1, concat_axis=0, tiled=True)
        pred = lax.psum_scatter(
            jnp.dot(blocks, expr, precision=lax.Precision.HIGHEST),
            "spot",
            scatter_dimension=0,
            tiled=True,
        )
        gene_dot = jnp.sum(valid[:, None] * pred * target, axis=0)
        gene_pred = jnp.sum(valid[:, None] * pred * pred, axis=0)
        gene_true = jnp.sum(valid[:, None] * target * target, axis=0)
        mass_part = jnp.sum(valid * mass)
        kcell = valid * counted
        cell_part = jnp.sum(kcell)
        spot_dot = jnp.sum(pred * target, axis=1)
        spot_pred = jnp.sum(pred * pred, axis=1)
        spot_true = jnp.sum(target * target, axis=1)
        gene_dot, gene_pred, gene_true, mass_total, cell_total = lax.psum(
            (gene_dot, gene_pred, gene_true, mass_part, cell_part), "spot"
        )
        spot_dot, spot_pred, spot_true = lax.psum((spot_dot, spot_pred, spot_true), "gene")
        gene_inv = lax.rsqrt(gene_pred * gene_true + tiny)
        cos_gene = gene_dot * gene_inv
        spot_inv = lax.rsqrt(spot_pred * spot_true + tiny)
        cos_spot = spot_dot * spot_inv
        share = kcell / cell_total
        scale_count = slide_spots[slide].astype(jnp.float32)
        kl_part = jnp.sum(
            share * (jnp.log(counted) - jnp.log(cell_total) - jnp.log(mass) + jnp.log(mass_total))
        )
        loss_local = loss_local - gene_share * jnp.sum(cos_gene)
        loss_local = loss_local + row_share * (scale_count * kl_part - jnp.sum(valid * cos_spot))
        gene_back = cos_gene * gene_true / (gene_pred * gene_true + tiny)
        spot_back = cos_spot * spot_true / (spot_pred * spot_true + tiny)
        dpred = -valid[:, None] * (
            target * (gene_inv[None, :] + spot_inv[:, None])
            - pred * gene_back[None, :]
            - pred * spot_back[:, None]
        )
        dmass = scale_count * valid * (1.0 / mass_total - share / mass)
        pred_list.append(pred)
        grads_full, mass_full = (
            lax.all_gather(dpred, "spot", axis=0, tiled=True),
            lax.all_gather(dmass, "spot", axis=0, tiled=True),
        )
        dprob_cells = jnp.dot(grads_full, expr.T, precision=lax.Precision.HIGHEST)
        dprob_cells = lax.psum(dprob_cells, "gene")
        expr_acc = expr_acc + lax.dot_general(
            blocks, grads_full, (((0,), (0,)), ((), ())), precision=lax.Precision.HIGHEST
        )
        dprob_cells = dprob_cells + mass_full[:, None] * own_weights[None, :]
        dprob_rows = lax.all_to_all(dprob_cells, "spot", split_axis=0, concat_axis=1, tiled=True)
        inner = jnp.sum(probs * dprob_rows, axis=1, keepdims=True)
        dlogit = probs * (dprob_rows - inner)
        grad_list.append(dlogit)
    loss = lax.psum(loss_local, ("spot", "gene"))
    return (jnp.stack(pred_list), loss, jnp.stack(grad_list), expr_acc)


def solution(mesh):
    places = mesh.shape["spot"]

    def on_device(logits, expr, spatial, slide_spots, spot_cells, cell_prior):
        if places == PLANE * PLANE and mesh.shape["gene"] == 2 and expr.shape[1] == sum(FORWARD):
            return plane_call(
                logits, expr, spatial, slide_spots, spot_cells, cell_prior, places // PLANE
            )
        return general_plan(logits, expr, spatial, slide_spots, spot_cells, cell_prior)

    in_specs = (
        P(None, "spot", None),
        P("spot", "gene"),
        P(None, "spot", "gene"),
        P(),
        P(None, "spot"),
        P(),
    )
    out_specs = (P(None, "spot", "gene"), P(), P(None, "spot", None), P("spot", "gene"))
    return jax.shard_map(
        on_device, mesh=mesh, in_specs=in_specs, out_specs=out_specs, check_vma=False
    )
```

```python
import functools

import jax
import jax.numpy as jnp
from jax import lax
from jax.experimental import pallas as pl
from jax.experimental.pallas import tpu as pltpu
from jax.sharding import PartitionSpec as P

tiny = 1e-06
fixed_point = 16384.0
F32 = jnp.float32
BF16 = jnp.bfloat16
MESH = pl.DeviceIdType.MESH

PLANE = 4
LANES = 128
STEP_ROWS = 16
BLOCK = 32
TALL = 256
FORWARD = (128, 256, 256, 128, 128, 128)
BACKWARD = (128, 128, 256, 256, 256)
SPLIT = 2
LEAD = 1
NEAR_LEAD = 3
EARLY = 3
STEPS = (
    ("far", 0),
    ("far", 1),
    ("near", 0),
    ("share",),
    ("far", 2),
    ("far", 3),
    ("take",),
    ("whole", 0),
    ("near", 1),
    ("product", 0),
    ("sum", 0),
    ("whole", 1),
    ("near", 2),
    ("product", 1),
    ("whole", 2),
    ("product", 2),
    ("whole", 3),
    ("near", 3),
    ("product", 3),
    ("far", 4),
    ("whole", 4),
    ("near", 4),
    ("product", 4),
    ("sum", 1),
    ("turn", 0),
    ("far", 5),
    ("whole", 5),
    ("near", 5),
    ("product", 5),
    ("sum", 2),
    ("plane", 0),
    ("turn", 1),
    ("sum", 3),
    ("line", 0),
    ("sum", 4),
    ("sum", 5),
    ("plane", 1),
    ("cores",),
    ("genes", 0),
    ("spots",),
    ("grad", 0),
    ("grad", 1),
    ("grad", 2),
    ("line", 1),
    ("backward", 0),
    ("backward", 1),
    ("add_near", 0),
    ("genes", 1),
    ("grad", 3),
    ("backward", 2),
    ("probs", 0),
    ("add_far", 0),
    ("probs", 1),
    ("expr", 0),
    ("grad", 4),
    ("add_near", 1),
    ("probs", 2),
    ("terms",),
    ("backward", 3),
    ("probs", 3),
    ("add_near", 2),
    ("backward", 4),
    ("add_far", 1),
    ("probs", 4),
    ("exchange",),
    ("add_near", 3),
    ("add_far", 2),
    ("left",),
    ("return",),
    ("loss",),
    ("add_far", 3),
    ("expr", 1),
    ("add_near", 4),
    ("logits",),
    ("add_far", 4),
    ("expr", 2),
    ("expr", 3),
    ("expr", 4),
)


def halves(value):
    high = value.astype(BF16)
    return high, (value - high.astype(F32)).astype(BF16)


def threefold(value):
    high, low = halves(value)
    return jnp.concatenate([high, high, low], axis=1)


def product(a, b, contract):
    return lax.dot_general(a, b, (contract, ((), ())), preferred_element_type=F32)


def plane_kernel(lines, forward_widths, backward_widths, *refs):
    chunks, turns = len(forward_widths), len(backward_widths)
    (
        (logits_ref, expr_ref, spatial_ref, count_in, cells_in, prior_in),
        (pr, loss_ref, glog, ge),
        (count_ref, cells_ref, prior_ref, lg, lq, tg, ex, pq, ab, af, probs_3, turned_3, expr_3, sacc, s1, s2, gv, ss, rowv, rs),
        (grad_3, factor, t0, p0, vr, fs, fx, fy, fz, fr, inn, l1, l2),
        (loc, ou_s, ou_r, od_s, od_r, fu_s, fu_r, fd_s, fd_r, a_s, a_r, a2_s, a2_r, r_s, r_r),
        (c_s, c_r, s1_s, s1_r, s2_s, s2_r, ss_s, ss_r, d_s, d_r, ru_s, ru_r, rd_s, rd_r),
        (f_s, f_r, fx_s, fx_r, go_s, go_r, in_s, in_r, l1_s, l1_r, l2_s, l2_r, t0_s, t0_r, p0_s, p0_r, vr_s, vr_r),
        bb,
        cs,
        cr,
        ds,
        es,
        ru,
        rd,
    ) = grouped(refs, (6, 4, 20, 13, 15, 14, 18, chunks, chunks, chunks, turns, turns, turns, turns))
    place = lax.axis_index("spot")
    core = lax.axis_index("gene")
    z = place // PLANE
    q = place % PLANE
    col, row = q % 2, q // 2
    diagonal, mate_x, mate_y = (1 - row) * 2 + 1 - col, row * 2 + 1 - col, (1 - row) * 2 + col
    mates = (mate_x + core * (mate_y - mate_x), diagonal, mate_y + core * (mate_x - mate_y))
    others = tuple((z + step) % lines for step in range(1, lines))
    up, down = (place + PLANE, core), (place - PLANE, core)
    sibling = (place, 1 - core)
    slides, slide_rows = logits_ref.shape[0], logits_ref.shape[1]
    rows = slides * slide_rows
    cb = expr_ref.shape[0]
    genes = expr_ref.shape[1]
    last = lines - 1

    def mate(p):
        return (z * PLANE + p, core)

    def send(src, dst, send_sem, recv_sem, device):
        copy = pltpu.make_async_remote_copy(
            src_ref=src, dst_ref=dst, send_sem=send_sem, recv_sem=recv_sem, device_id=device, device_id_type=MESH
        )
        copy.start()

    def arrived(dst, recv_sem):
        pltpu.make_async_copy(dst, dst, recv_sem).wait()

    sent = arrived

    def cols(k):
        return pl.ds(sum(forward_widths[:k]), forward_widths[k])

    def turn_cols(k):
        return pl.ds(sum(backward_widths[:k]), backward_widths[k])

    def block(index):
        return pl.ds(pl.multiple_of(index * cb, cb), cb)

    def share(index):
        return pl.ds(pl.multiple_of(index * rows, rows), rows)

    def half(index):
        return pl.ds(pl.multiple_of(index * slide_rows, slide_rows), slide_rows)

    small = ((prior_in, prior_ref), (count_in, count_ref), (cells_in, cells_ref))
    pltpu.make_async_copy(expr_ref, ex, loc.at[2 * slides]).start()
    for m in range(slides):
        pltpu.make_async_copy(logits_ref.at[m], lg.at[half(m)], loc.at[m]).start()
    for at, (src, dst) in enumerate(small):
        pltpu.make_async_copy(src, dst, loc.at[2 * slides + 1 + at]).start()
    for m in range(slides):
        pltpu.make_async_copy(spatial_ref.at[m], tg.at[half(m)], loc.at[slides + m]).start()

    barrier = pltpu.get_barrier_semaphore()
    for p in mates:
        pl.semaphore_signal(barrier, inc=1, device_id=mate(p), device_id_type=MESH)
    for o in others:
        pl.semaphore_signal(barrier, inc=1, device_id=(o * PLANE + q, core), device_id_type=MESH)
    pl.semaphore_signal(barrier, inc=1, device_id=sibling, device_id_type=MESH)
    pltpu.make_async_copy(expr_ref, ex, loc.at[2 * slides]).wait()
    for k in range(chunks):
        bb[k][block(z), :] = ex[:, cols(k)]
    for m in range(slides):
        pltpu.make_async_copy(logits_ref.at[m], lg.at[half(m)], loc.at[m]).wait()
    for p in range(PLANE):
        for line in range(lines):
            lq[p, :, pl.ds(line * cb, cb)] = lg[half(core), pl.ds((line * PLANE + p) * cb, cb)]
    pl.semaphore_wait(barrier, len(mates) + len(others) + 1)

    def own_up(k):
        here = bb[k].at[block(z)]
        send(here, here, ou_s.at[k], ou_r.at[k], up)

    def own_down(k):
        here = bb[k].at[block(z)]
        send(here, here, od_s.at[k], od_r.at[k], down)

    def low(at):
        return 2 * at < lines

    for at in range(lines):

        @pl.when(z == at)
        def _():
            for k in range(chunks):
                if at < last and (at == 0 or k < (LEAD if low(at) else NEAR_LEAD)):
                    own_up(k)
                if at > 0 and (at == last or k < (NEAR_LEAD if low(at) else LEAD)):
                    own_down(k)

    for p in mates:
        send(lq.at[p], ab.at[q, half(core)], a_s, a_r.at[q], mate(p))

    def from_below(k, at):
        arrived(bb[k].at[pl.ds((at - 1) * cb, cb)], ou_r.at[k])
        if at > 1:
            arrived(bb[k].at[pl.ds(0, (at - 1) * cb)], fu_r.at[k])

    def from_above(k, at):
        arrived(bb[k].at[pl.ds((at + 1) * cb, cb)], od_r.at[k])
        if at < last - 1:
            arrived(bb[k].at[pl.ds((at + 2) * cb, (last - 1 - at) * cb)], fd_r.at[k])

    def upward(k, at):
        from_below(k, at)
        here = bb[k].at[pl.ds(0, at * cb)]
        send(here, here, fu_s.at[k], fu_r.at[k], up)

    def downward(k, at):
        from_above(k, at)
        here = bb[k].at[pl.ds((at + 1) * cb, (last - at) * cb)]
        send(here, here, fd_s.at[k], fd_r.at[k], down)

    def forward_far(k):
        for at in range(1, last):

            @pl.when(z == at)
            def _():
                (upward if low(at) else downward)(k, at)
                if k + LEAD < chunks:
                    (own_up if low(at) else own_down)(k + LEAD)

    def forward_near(k):
        for at in range(1, last):

            @pl.when(z == at)
            def _():
                (downward if low(at) else upward)(k, at)
                if k + NEAR_LEAD < chunks:
                    (own_down if low(at) else own_up)(k + NEAR_LEAD)

    def gathered(k):
        @pl.when(z == 0)
        def _():
            from_above(k, 0)

        @pl.when(z == last)
        def _():
            from_below(k, last)

    for at, (src, dst) in enumerate(small):
        pltpu.make_async_copy(src, dst, loc.at[2 * slides + 1 + at]).wait()
    weights = prior_ref[...].astype(F32) / fixed_point

    @pl.loop(0, rows // STEP_ROWS)
    def _(step):
        at = pl.ds(pl.multiple_of(step * STEP_ROWS, STEP_ROWS), STEP_ROWS)
        value = lg[at, :]
        peak = jnp.max(value, axis=1, keepdims=True)
        raised = jnp.exp(value - peak)
        scale = 1.0 / jnp.sum(raised, axis=1, keepdims=True)
        probs = raised * scale
        mass_rows = jnp.sum(probs * weights, axis=1, keepdims=True)
        rowv[0, at, :] = jnp.broadcast_to(mass_rows, (STEP_ROWS, LANES))
        rowv[1, at, :] = jnp.broadcast_to(peak, (STEP_ROWS, LANES))
        rowv[2, at, :] = jnp.broadcast_to(scale, (STEP_ROWS, LANES))
        for p in range(PLANE):
            for line in range(lines):
                at_cells = (line * PLANE + p) * cb
                pq[p, at, pl.ds(line * cb, cb)] = probs[:, at_cells : at_cells + cb]

    wide = lax.broadcasted_iota(jnp.int32, (rows, LANES), 1)
    rs[q] = jnp.where(wide == 0, rowv[1], rowv[2]).T[0:8]
    for p in mates:
        send(rs.at[q], rs.at[q], r_s, r_r.at[q], mate(p))

    rid = lax.broadcasted_iota(jnp.int32, (rows, 1), 0)
    first = rid < slide_rows
    position = place * slide_rows + jnp.where(first, rid, rid - slide_rows)
    count = jnp.where(first, count_ref[0], count_ref[1])
    valid = (position < count).astype(F32)
    scale_count = count.astype(F32)
    square = (slide_rows, slide_rows)
    eye = lax.broadcasted_iota(jnp.int32, square, 0) == lax.broadcasted_iota(jnp.int32, square, 1)
    counted = jnp.concatenate(
        [
            jnp.sum(jnp.where(eye, cells_ref[m : m + 1, :].astype(F32), 0.0), axis=1, keepdims=True)
            for m in range(slides)
        ],
        axis=0,
    )
    mass = rowv[0, :, 0:1]
    kcell = valid * counted

    def by_slide(value):
        return [jnp.sum(value[m * slide_rows : (m + 1) * slide_rows], axis=0, keepdims=True) for m in range(slides)]

    mass_parts = by_slide(valid * mass)
    cell_parts = by_slide(kcell)
    lane = lax.broadcasted_iota(jnp.int32, (1, LANES), 1)
    scalars = jnp.zeros((1, LANES), F32)
    for at, value in enumerate(mass_parts + cell_parts):
        scalars = jnp.where(lane == at, value, scalars)
    for m in range(slides):
        pltpu.make_async_copy(spatial_ref.at[m], tg.at[half(m)], loc.at[slides + m]).wait()

    head = backward_widths[0]
    t0[q] = tg[:, 0:head]
    for p in mates:
        send(t0.at[q], t0.at[q], t0_s, t0_r.at[q], mate(p))
    sacc[...] = jnp.zeros_like(sacc)
    s1[q, 3 * slides :, :] = jnp.zeros((8 - 3 * slides, genes), F32)
    s1[q, 3 * slides : 3 * slides + 1, 0:LANES] = scalars

    def share_logits():
        for p in mates:
            here = ab.at[p, half(core)]
            arrived(here, a_r.at[p])
            send(here, here, a2_s, a2_r.at[p], sibling)

    def lay_probs(p, at, value):
        af[p, at, :] = value
        there = pl.ds(pl.multiple_of(p * rows + at.start, BLOCK), BLOCK)
        probs_3[there, :] = threefold(value)

    def take_probs():
        in_blocks(0, rows, lambda at: lay_probs(q, at, pq[q, at, :]))
        for p in mates:
            arrived(rs.at[p], r_r.at[p])
            arrived(ab.at[p, half(1 - core)], a2_r.at[p])
            rowv[1] = jnp.concatenate([rs[p].T, jnp.zeros((rows, LANES - 8), F32)], axis=1)

            def take(at):
                probs = jnp.exp(ab[p, at, :] - rowv[1, at, 0:1]) * rowv[1, at, 1:2]
                lay_probs(p, at, probs)

            in_blocks(0, rows, take)

    def transpose(part):
        @pl.loop(0, PLANE // 2)
        def _(step):
            p = part * (PLANE // 2) + step
            high, low_part = halves(af[p].T)
            for third, value in enumerate((high, high, low_part)):
                turned_3[:, pl.ds(pl.multiple_of(third * PLANE * rows + p * rows, rows), rows)] = value

    def in_blocks(start, count, body):
        @pl.loop(0, count // BLOCK)
        def _(step):
            body(pl.ds(pl.multiple_of(start + step * BLOCK, BLOCK), BLOCK))

    quarter = lines * cb

    def lay_factor(at, length, width, value):
        high, low_part = halves(value)
        for third, part in enumerate((high, low_part, high)):
            here = pl.ds(pl.multiple_of(third * length + at.start, BLOCK), BLOCK)
            factor[here, 0:width] = part

    def keep_expr(k, at, value):
        start = sum(forward_widths[:k])
        for turn in range(turns):
            origin, width = sum(backward_widths[:turn]), backward_widths[turn]
            lo, hi = max(start, origin), min(start + forward_widths[k], origin + width)
            if lo < hi:
                high, low_part = halves(value[:, lo - start : hi - start])
                for third, part in enumerate((high, low_part, high)):
                    expr_3[at, pl.ds(3 * origin + third * width + lo - origin, hi - lo)] = part

    def three_turn_cols(k):
        return pl.ds(3 * sum(backward_widths[:k]), 3 * backward_widths[k])

    def forward_product(k):
        width = forward_widths[k]

        def lay(at):
            value = bb[k][at, :]
            lay_factor(at, quarter, width, value)
            keep_expr(k, at, value)

        in_blocks(0, quarter, lay)
        if k < chunks - 1:

            @pl.loop(0, PLANE * rows // TALL)
            def _(step):
                tall = pl.ds(pl.multiple_of(step * TALL, TALL), TALL)
                cs[k][tall, :] = product(probs_3[tall, :], factor[0 : 3 * quarter, 0:width], ((1,), (0,)))

            for p in mates:
                pass_pred(k, p)
        else:
            for side, served in ((1 - row, (diagonal, mate_y)), (row, (mate_x,))):
                pair = pl.ds(pl.multiple_of(2 * side * rows, 2 * rows), 2 * rows)
                cs[k][pair, :] = product(probs_3[pair, :], factor[0 : 3 * quarter, 0:width], ((1,), (0,)))
                for p in served:
                    pass_pred(k, p)

    def pass_pred(k, p):
        send(cs[k].at[share(p)], cr[k].at[q], c_s.at[k], c_r.at[k, q], mate(p))

    def finish_pred(k):
        total = cs[k][share(q), :]
        for p in mates:
            arrived(cr[k].at[p], c_r.at[k, p])
            total = total + cr[k][p]
        pr[:, cols(k)] = total
        if k == 0:
            p0[q] = total[:, 0:head]
            for p in mates:
                send(p0.at[q], p0.at[q], p0_s, p0_r.at[q], mate(p))
        truth = tg[:, cols(k)]
        for at, value in enumerate((total * truth, total * total, truth * truth)):
            sacc[at] += lane_groups(value)
        kept = valid * total
        stats = by_slide(kept * truth) + by_slide(kept * total) + by_slide(valid * truth * truth)
        s1[q, 0 : 3 * slides, cols(k)] = jnp.concatenate(stats, axis=0)

    early = sum(forward_widths[:EARLY])
    parts = (pl.ds(0, early), pl.ds(early, genes - early))

    def sum_plane(at):
        for p in mates:
            send(s1.at[q, :, parts[at]], s1.at[q, :, parts[at]], s1_s, s1_r.at[at, q], mate(p))

    def sum_line(at):
        for p in mates:
            arrived(s1.at[p, :, parts[at]], s1_r.at[at, p])
        s2[z, :, parts[at]] = (s1[0, :, parts[at]] + s1[1, :, parts[at]]) + (s1[2, :, parts[at]] + s1[3, :, parts[at]])
        for o in others:
            send(s2.at[z, :, parts[at]], s2.at[z, :, parts[at]], s2_s, s2_r.at[at, z], (o * PLANE + q, core))

    kept = {}

    def finish_genes(at):
        for o in others:
            arrived(s2.at[o, :, parts[at]], s2_r.at[at, o])
        total = s2[0, :, parts[at]]
        for line in range(1, lines):
            total = total + s2[line, :, parts[at]]
        gene_dot, gene_pred, gene_true = total[0:2], total[2:4], total[4:6]
        gene_inv = lax.rsqrt(gene_pred * gene_true + tiny)
        cos_gene = gene_dot * gene_inv
        gv[0:2, parts[at]] = gene_inv
        gv[2:4, parts[at]] = cos_gene * gene_true / (gene_pred * gene_true + tiny)
        kept["genes", at] = jnp.sum(jnp.sum(cos_gene, axis=1, keepdims=True), axis=0, keepdims=True)
        if at == 0:
            kept["mass"] = jnp.where(first, total[6:7, 0:1], total[6:7, 1:2])
            kept["cells"] = jnp.where(first, total[6:7, 2:3], total[6:7, 3:4])

    def sum_cores():
        sums = [jnp.sum(sacc[at], axis=1, keepdims=True) for at in range(3)]
        ss[core] = jnp.where(wide == 0, sums[0], jnp.where(wide == 1, sums[1], sums[2])).T[0:8]
        send(ss.at[core], ss.at[core], ss_s, ss_r, sibling)

    def finish_spots():
        lane_id = lax.broadcasted_iota(jnp.int32, (1, rows), 1)
        first_lane = lane_id < slide_rows
        lane_position = place * slide_rows + jnp.where(first_lane, lane_id, lane_id - slide_rows)
        lane_valid = (lane_position < jnp.where(first_lane, count_ref[0], count_ref[1])).astype(F32)
        arrived(ss.at[1 - core], ss_r)
        spot = ss[0] + ss[1]
        spot_dot, spot_pred, spot_true = spot[0:1], spot[1:2], spot[2:3]
        spot_inv = lax.rsqrt(spot_pred * spot_true + tiny)
        cos_spot = spot_dot * spot_inv
        spot_back = cos_spot * spot_true / (spot_pred * spot_true + tiny)
        kept["cos"] = jnp.sum(lane_valid * cos_spot, axis=1, keepdims=True)
        vectors = [lane_valid * spot_inv, lane_valid * spot_back, lane_valid, jnp.zeros((5, rows), F32)]
        vr[q] = jnp.concatenate(vectors, axis=0)
        sacc[0] = jnp.zeros_like(sacc[0])

    def gradient(truth, guess, by_row, k):
        pieces = []
        for m in range(slides):
            lo, hi = m * slide_rows, (m + 1) * slide_rows
            inverse, back = gv[m : m + 1, turn_cols(k)], gv[2 + m : 3 + m, turn_cols(k)]
            spot_inv, spot_back, spot_valid = by_row[lo:hi, 0:1], by_row[lo:hi, 1:2], by_row[lo:hi, 2:3]
            pieces.append(
                guess[lo:hi] * (spot_valid * back + spot_back) - truth[lo:hi] * (spot_valid * inverse + spot_inv)
            )
        return jnp.concatenate(pieces, axis=0)

    def head_gradient():
        for p in mates:
            arrived(t0.at[p], t0_r.at[p])
            arrived(p0.at[p], p0_r.at[p])
            arrived(vr.at[p], vr_r.at[p])
        for p in range(PLANE):
            ds[0][share(p), :] = gradient(t0[p], p0[p], vr[p].T, 0)
        sacc[0] += lane_groups(ds[0][share(q), :] * p0[q])

    def send_grad(k):
        if k == 0:
            for p in mates:
                send(vr.at[q], vr.at[q], vr_s, vr_r.at[q], mate(p))
            kept["by_row"] = vr[q].T
            return
        grad = gradient(tg[:, turn_cols(k)], pr[:, turn_cols(k)], kept["by_row"], k)
        here = ds[k].at[share(q)]
        here[...] = grad
        for p in mates:
            send(here, here, d_s.at[k], d_r.at[k, q], mate(p))
        sacc[0] += lane_groups(grad * pr[:, turn_cols(k)])

    def send_terms():
        mass_total, cell_total = kept["mass"], kept["cells"]
        portion = kcell / cell_total
        kl_rows = portion * (jnp.log(counted) - jnp.log(cell_total) - jnp.log(mass) + jnp.log(mass_total))
        dmass = scale_count * valid * (1.0 / mass_total - portion / mass)
        terms = jnp.sum(scale_count * kl_rows, axis=0, keepdims=True) - kept["cos"]
        l1[q] = jnp.broadcast_to(terms, (8, LANES))
        for p in mates:
            send(l1.at[q], l1.at[q], l1_s, l1_r.at[q], mate(p))
        inner = jnp.sum(sacc[0], axis=1, keepdims=True)
        inn[core] = jnp.where(wide == 0, inner, kept["genes", 0] + kept["genes", 1])
        send(inn.at[core], inn.at[core], in_s, in_r, sibling)
        rowv[1] = jnp.broadcast_to(dmass, (rows, LANES))

    middle = lines // 2

    def backward_product(k):
        if k == 0:
            head_gradient()
        else:
            for p in mates:
                arrived(ds[k].at[share(p)], d_r.at[k, p])
        width, spots = backward_widths[k], PLANE * rows

        def lay(at):
            value = ds[k][at, :]
            lay_factor(at, spots, width, value)
            grad_3[at, three_turn_cols(k)] = threefold(value)

        in_blocks(0, spots, lay)
        if not halved(k):

            @pl.loop(0, quarter // TALL)
            def _(step):
                tall = pl.ds(pl.multiple_of(step * TALL, TALL), TALL)
                es[k][tall, :] = product(turned_3[tall, :], factor[0 : 3 * spots, 0:width], ((1,), (0,)))

        for turn in range(2):
            if halved(k):
                side = (1 - z // middle) if turn == 0 else z // middle
                pair = pl.ds(pl.multiple_of(side * middle * cb, middle * cb), middle * cb)
                es[k][pair, :] = product(turned_3[pair, :], factor[0 : 3 * spots, 0:width], ((1,), (0,)))

            @pl.when(z == 0)
            def _():
                if halved(k):
                    pass_up(k, middle if turn == 0 else 1, middle if turn == 0 else middle - 1, turn)
                elif whole(k):
                    if turn == 0:
                        pass_up(k, 1, last, 0)
                elif turn == 0:
                    for line in range(last, 0, -1):
                        pass_up(k, line, 1, line)

            @pl.when(z == last)
            def _():
                if halved(k):
                    pass_down(k, 0 if turn == 0 else middle, middle if turn == 0 else middle - 1, turn)
                elif whole(k):
                    if turn == 0:
                        pass_down(k, 0, last, 0)
                elif turn == 0:
                    for line in range(last):
                        pass_down(k, line, 1, line)

    def halved(k):
        return k == 0

    def whole(k):
        return 0 < k < turns - SPLIT

    def pass_up(k, line, count, slot):
        here = pl.ds(line * cb, count * cb)
        send(es[k].at[here], ru[k].at[here], ru_s.at[k], ru_r.at[k, slot], up)

    def pass_down(k, line, count, slot):
        here = pl.ds(line * cb, count * cb)
        send(es[k].at[here], rd[k].at[here], rd_s.at[k], rd_r.at[k, slot], down)

    def take_up(k, line, count, slot):
        arrived(ru[k].at[pl.ds(line * cb, count * cb)], ru_r.at[k, slot])

    def take_down(k, line, count, slot):
        arrived(rd[k].at[pl.ds(line * cb, count * cb)], rd_r.at[k, slot])

    def add_up(k, line, count):
        def add(at):
            es[k][at, :] += ru[k][at, :]

        in_blocks(line * cb, count * cb, add)

    def add_down(k, line, count):
        def add(at):
            es[k][at, :] += rd[k][at, :]

        in_blocks(line * cb, count * cb, add)

    def rising(k, at):
        if halved(k) or whole(k):
            start = middle if halved(k) else at
            take_up(k, start, lines - start, 0)
            above = max(at + 1, start)
            add_up(k, above, lines - above)
            pass_up(k, above, lines - above, 0)
        else:
            for line in range(last, at, -1):
                take_up(k, line, 1, line)
                add_up(k, line, 1)
                pass_up(k, line, 1, line)

    def falling(k, at):
        if halved(k) or whole(k):
            end = middle if halved(k) else at + 1
            take_down(k, 0, end, 0)
            below = min(at, end)
            add_down(k, 0, below)
            pass_down(k, 0, below, 0)
        else:
            for line in range(at):
                take_down(k, line, 1, line)
                add_down(k, line, 1)
                pass_down(k, line, 1, line)

    def add_near(k):
        for at in range(1, last):

            @pl.when(z == at)
            def _():
                (rising if low(at) else falling)(k, at)

    def add_far(k):
        for at in range(1, last):

            @pl.when(z == at)
            def _():
                (falling if low(at) else rising)(k, at)

    def finish_expr(k):
        for at in range(lines):

            @pl.when(z == at)
            def _():
                if at > 0:
                    if halved(k) and at < middle:
                        take_up(k, at, 1, 1)
                    elif at == last and (halved(k) or whole(k)):
                        take_up(k, at, 1, 0)
                    elif not halved(k) and not whole(k):
                        take_up(k, at, 1, at)
                if at < last:
                    if halved(k) and at >= middle:
                        take_down(k, at, 1, 1)
                    elif at == 0 and (halved(k) or whole(k)):
                        take_down(k, at, 1, 0)
                    elif not halved(k) and not whole(k):
                        take_down(k, at, 1, at)

        from_low, from_high = z > 0, z < last

        @pl.loop(0, cb // BLOCK)
        def _(step):
            here = pl.ds(pl.multiple_of(step * BLOCK, BLOCK), BLOCK)
            own = pl.ds(pl.multiple_of(z * cb + step * BLOCK, BLOCK), BLOCK)
            total = es[k][own, :]
            total = total + jnp.where(from_low, ru[k][own, :], 0.0)
            ge[here, turn_cols(k)] = total + jnp.where(from_high, rd[k][own, :], 0.0)

    def probs_gradient(k):
        at = three_turn_cols(k)

        @pl.loop(0, PLANE * rows // TALL)
        def _(step):
            tall = pl.ds(pl.multiple_of(step * TALL, TALL), TALL)
            part = product(grad_3[tall, at], expr_3[:, at], ((1,), (1,)))
            if k == 0:
                fs[tall, :] = part
            else:
                fs[tall, :] += part

    def slide_of(p, m):
        return pl.ds(pl.multiple_of(p * rows + m * slide_rows, slide_rows), slide_rows)

    def sum_probs_cores():
        for p in mates + (q,):
            fx[p] = fs[slide_of(p, 1 - core), :]
            send(fx.at[p], fy.at[p], fx_s, fx_r.at[p], sibling)

    def return_probs():
        for p in mates:
            arrived(fy.at[p], fx_r.at[p])
            fz[p] = fs[slide_of(p, core), :] + fy[p]
            send(fz.at[p], fr.at[q], f_s, f_r.at[q], mate(p))
        arrived(fy.at[q], fx_r.at[q])
        fr[q] = fs[slide_of(q, core), :] + fy[q]

    def pass_terms():
        for p in mates:
            arrived(l1.at[p], l1_r.at[p])
        l2[z] = (l1[0] + l1[1]) + (l1[2] + l1[3])
        for o in others:
            send(l2.at[z], l2.at[z], l2_s, l2_r.at[z], (o * PLANE + q, core))

    def part_of(slide, m):
        start = slide * slide_rows + m * (slide_rows // 2)
        return pl.ds(pl.multiple_of(start, slide_rows // 2), slide_rows // 2)

    def finish_logits():
        arrived(inn.at[1 - core], in_r)
        rowv[2] = (inn[0] + inn[1]) + rowv[1] * rowv[0]
        for p in mates:
            arrived(fr.at[p], f_r.at[p])
        for m in range(2):

            @pl.loop(0, slide_rows // STEP_ROWS // 2)
            def _(step):
                row_at = (m * (slide_rows // STEP_ROWS // 2) + step) * STEP_ROWS
                at = pl.ds(pl.multiple_of(row_at, STEP_ROWS), STEP_ROWS)
                whole_at = pl.ds(pl.multiple_of(core * slide_rows + row_at, STEP_ROWS), STEP_ROWS)
                by_mass, total_inner = rowv[1, whole_at, 0:1], rowv[2, whole_at, 0:1]
                for p in range(PLANE):
                    for line in range(lines):
                        here, there = pl.ds(line * cb, cb), (line * PLANE + p) * cb
                        grad = fr[p, at, here] + by_mass * weights[:, there : there + cb]
                        glog[whole_at, pl.ds(there, cb)] = pq[p, whole_at, here] * (grad - total_inner)

            here = part_of(core, m)
            send(glog.at[here], glog.at[here], go_s, go_r.at[m], sibling)

    def forward_left():
        for k in range(chunks):

            @pl.when(z < last)
            def _():
                sent(bb[k].at[block(z)], ou_s.at[k])

            @pl.when(z > 0)
            def _():
                sent(bb[k].at[block(z)], od_s.at[k])

            for at in range(1, last):

                @pl.when(z == at)
                def _():
                    sent(bb[k].at[pl.ds(0, at * cb)], fu_s.at[k])
                    sent(bb[k].at[pl.ds((at + 1) * cb, (last - at) * cb)], fd_s.at[k])

        three = pl.ds(0, len(mates))
        sent(ab.at[three, half(0)], a_s)
        sent(ab.at[three, half(0)], a2_s)
        sent(rs.at[three], r_s)
        sent(t0.at[three], t0_s)
        sent(p0.at[three], p0_s)
        for k in range(chunks):
            sent(cr[k].at[three], c_s.at[k])
        sent(s1.at[three], s1_s)
        sent(s2.at[pl.ds(0, last)], s2_s)
        sent(ss.at[0], ss_s)

    steps = {
        "far": forward_far,
        "near": forward_near,
        "share": share_logits,
        "take": take_probs,
        "whole": gathered,
        "product": forward_product,
        "sum": finish_pred,
        "turn": transpose,
        "plane": sum_plane,
        "line": sum_line,
        "genes": finish_genes,
        "cores": sum_cores,
        "spots": finish_spots,
        "grad": send_grad,
        "terms": send_terms,
        "backward": backward_product,
        "probs": probs_gradient,
        "exchange": sum_probs_cores,
        "return": return_probs,
        "loss": pass_terms,
        "logits": finish_logits,
        "add_near": add_near,
        "add_far": add_far,
        "expr": finish_expr,
        "left": forward_left,
    }
    for name, *where in STEPS:
        steps[name](*where)

    for o in others:
        arrived(l2.at[o], l2_r.at[o])
    loss = l2[0]
    for line in range(1, lines):
        loss = loss + l2[line]
    loss_ref[...] = loss[0:1, 0:1] - (inn[0, 0:1, 1:2] + inn[1, 0:1, 1:2])
    for m in range(2):
        arrived(glog.at[part_of(1 - core, m)], go_r.at[m])

    for k in range(turns):
        for at in range(lines):

            @pl.when(z == at)
            def _():
                if at < last:
                    sent(es[k].at[pl.ds((at + 1) * cb, (last - at) * cb)], ru_s.at[k])
                if at > 0:
                    sent(es[k].at[pl.ds(0, at * cb)], rd_s.at[k])

    three = pl.ds(0, len(mates))
    for k in range(1, turns):
        sent(ds[k].at[pl.ds(0, len(mates) * rows)], d_s.at[k])
    sent(vr.at[three], vr_s)
    sent(inn.at[0], in_s)
    sent(l1.at[three], l1_s)
    sent(l2.at[pl.ds(0, last)], l2_s)
    sent(fr.at[three], f_s)
    sent(fx, fx_s)
    sent(glog.at[half(0)], go_s)


def lane_groups(value):
    parts = [value[:, at : at + LANES] for at in range(0, value.shape[1], LANES)]
    return functools.reduce(lambda a, b: a + b, parts)


def grouped(refs, sizes):
    at = 0
    for size in sizes:
        yield refs[at : at + size]
        at += size


def deliver(pred_in, loss_in, glog_in, gexp_in, pred_ref, loss_ref, glog_ref, gexp_ref, sems):
    slides, slide_rows = pred_ref.shape[0], pred_ref.shape[1]
    pairs = [(gexp_in, gexp_ref), (loss_in, loss_ref)]
    for m in range(slides):
        part = pl.ds(m * slide_rows, slide_rows)
        pairs += [(glog_in.at[part], glog_ref.at[m]), (pred_in.at[part], pred_ref.at[m])]
    copies = [pltpu.make_async_copy(src, dst, sems.at[at]) for at, (src, dst) in enumerate(pairs)]
    for copy in copies:
        copy.start()
    for copy in copies:
        copy.wait()


def plane_call(logits, expr, spatial, slide_spots, spot_cells, cell_prior, lines):
    slides, slide_rows, cells = logits.shape
    rows = slides * slide_rows
    cb, genes = expr.shape
    quarter = lines * cb
    spots = PLANE * rows
    chunks, turns = len(FORWARD), len(BACKWARD)
    dma = pltpu.SemaphoreType.DMA
    vmem = pltpu.VMEM
    anywhere = pl.BlockSpec(memory_space=pl.ANY)
    in_vmem = pl.BlockSpec(memory_space=pltpu.VMEM)
    scratch = [
        pltpu.SMEM((slides,), jnp.int32),
        vmem((slides, slide_rows), jnp.int32),
        vmem((1, cells), jnp.int32),
        vmem((rows, cells), F32),
        vmem((PLANE, slide_rows, quarter), F32),
        vmem((rows, genes), F32),
        vmem((cb, genes), F32),
        vmem((PLANE, rows, quarter), F32),
        vmem((PLANE, rows, quarter), F32),
        vmem((PLANE, rows, quarter), F32),
        vmem((spots, 3 * quarter), BF16),
        vmem((quarter, 3 * spots), BF16),
        vmem((quarter, 3 * genes), BF16),
        vmem((3, rows, LANES), F32),
        vmem((PLANE, 8, genes), F32),
        vmem((lines, 8, genes), F32),
        vmem((8, genes), F32),
        vmem((2, 8, rows), F32),
        vmem((3, rows, LANES), F32),
        vmem((PLANE, 8, rows), F32),
        vmem((spots, 3 * genes), BF16),
        vmem((3 * max(quarter, spots), max(FORWARD + BACKWARD)), BF16),
        vmem((PLANE, rows, BACKWARD[0]), F32),
        vmem((PLANE, rows, BACKWARD[0]), F32),
        vmem((PLANE, 8, rows), F32),
        vmem((spots, quarter), F32),
        vmem((PLANE, slide_rows, quarter), F32),
        vmem((PLANE, slide_rows, quarter), F32),
        vmem((PLANE, slide_rows, quarter), F32),
        vmem((PLANE, slide_rows, quarter), F32),
        vmem((2, rows, LANES), F32),
        vmem((PLANE, 8, LANES), F32),
        vmem((lines, 8, LANES), F32),
        dma((2 * slides + 4,)),
        dma((chunks,)),
        dma((chunks,)),
        dma((chunks,)),
        dma((chunks,)),
        dma((chunks,)),
        dma((chunks,)),
        dma((chunks,)),
        dma((chunks,)),
        dma,
        dma((PLANE,)),
        dma,
        dma((PLANE,)),
        dma,
        dma((PLANE,)),
        dma((chunks,)),
        dma((chunks, PLANE)),
        dma,
        dma((2, PLANE)),
        dma,
        dma((2, lines)),
        dma,
        dma,
        dma((turns,)),
        dma((turns, PLANE)),
        dma((turns,)),
        dma((turns, lines)),
        dma((turns,)),
        dma((turns, lines)),
        dma,
        dma((PLANE,)),
        dma,
        dma((PLANE,)),
        dma,
        dma((2,)),
        dma,
        dma,
        dma,
        dma((PLANE,)),
        dma,
        dma((lines,)),
        dma,
        dma((PLANE,)),
        dma,
        dma((PLANE,)),
        dma,
        dma((PLANE,)),
    ]
    for shape, widths in (
        ((quarter,), FORWARD),
        ((spots,), FORWARD),
        ((PLANE, rows), FORWARD),
        ((spots,), BACKWARD),
        ((quarter,), BACKWARD),
        ((quarter,), BACKWARD),
        ((quarter,), BACKWARD),
    ):
        scratch += [vmem(shape + (width,), F32) for width in widths]
    in_hbm = functools.partial(pltpu.with_memory_space_constraint, memory_space=pltpu.HBM)
    in_place = functools.partial(pltpu.with_memory_space_constraint, memory_space=pltpu.VMEM)
    results = pl.pallas_call(
        functools.partial(plane_kernel, lines, FORWARD, BACKWARD),
        out_shape=(
            vmem((rows, genes), F32),
            vmem((1, 1), F32),
            vmem((rows, cells), F32),
            vmem((cb, genes), F32),
        ),
        in_specs=[anywhere] * 6,
        out_specs=(in_vmem,) * 4,
        scratch_shapes=scratch,
        compiler_params=pltpu.CompilerParams(
            collective_id=0, has_side_effects=True, vmem_limit_bytes=48 * 1024 * 1024
        ),
    )(*map(in_hbm, (logits, expr, spatial, slide_spots, spot_cells, cell_prior.reshape(1, cells))))
    pred, loss, grad_logits, grad_expr = pl.pallas_call(
        deliver,
        out_shape=(
            jax.ShapeDtypeStruct((slides, slide_rows, genes), F32),
            jax.ShapeDtypeStruct((1, 1), F32),
            jax.ShapeDtypeStruct((slides, slide_rows, cells), F32),
            jax.ShapeDtypeStruct((cb, genes), F32),
        ),
        in_specs=[anywhere] * 4,
        out_specs=(anywhere,) * 4,
        scratch_shapes=[dma((2 * slides + 2,))],
        compiler_params=pltpu.CompilerParams(vmem_limit_bytes=4 * 1024 * 1024),
    )(*map(in_place, results))
    return pred, loss.reshape(()), grad_logits, grad_expr


def general_plan(logits, expr, spatial, slide_spots, spot_cells, cell_prior):
    place = lax.axis_index("spot")
    side = lax.axis_index("gene")
    rows_all = logits.shape[1]
    cell_rows = expr.shape[0]
    weights = cell_prior.astype(jnp.float32) / fixed_point
    gene_share = (place == 0).astype(jnp.float32)
    row_share = (side == 0).astype(jnp.float32)
    own_weights = lax.dynamic_slice_in_dim(weights, place * cell_rows, cell_rows, 0)
    expr_acc = jnp.zeros((cell_rows, expr.shape[1]), jnp.float32)
    loss_local = jnp.zeros((), jnp.float32)
    pred_list = []
    grad_list = []
    for slide in range(logits.shape[0]):
        logit_rows = logits[slide]
        counted = spot_cells[slide].astype(jnp.float32)
        target = spatial[slide]
        positions = place * rows_all + jnp.arange(rows_all, dtype=jnp.int32)
        valid = (positions < slide_spots[slide]).astype(jnp.float32)
        peak = jnp.max(logit_rows, axis=1, keepdims=True)
        raised = jnp.exp(logit_rows - peak)
        probs = raised / jnp.sum(raised, axis=1, keepdims=True)
        mass = jnp.dot(probs, weights, precision=lax.Precision.HIGHEST)
        blocks = lax.all_to_all(probs, "spot", split_axis=1, concat_axis=0, tiled=True)
        pred = lax.psum_scatter(
            jnp.dot(blocks, expr, precision=lax.Precision.HIGHEST),
            "spot",
            scatter_dimension=0,
            tiled=True,
        )
        gene_dot = jnp.sum(valid[:, None] * pred * target, axis=0)
        gene_pred = jnp.sum(valid[:, None] * pred * pred, axis=0)
        gene_true = jnp.sum(valid[:, None] * target * target, axis=0)
        mass_part = jnp.sum(valid * mass)
        kcell = valid * counted
        cell_part = jnp.sum(kcell)
        spot_dot = jnp.sum(pred * target, axis=1)
        spot_pred = jnp.sum(pred * pred, axis=1)
        spot_true = jnp.sum(target * target, axis=1)
        gene_dot, gene_pred, gene_true, mass_total, cell_total = lax.psum(
            (gene_dot, gene_pred, gene_true, mass_part, cell_part), "spot"
        )
        spot_dot, spot_pred, spot_true = lax.psum((spot_dot, spot_pred, spot_true), "gene")
        gene_inv = lax.rsqrt(gene_pred * gene_true + tiny)
        cos_gene = gene_dot * gene_inv
        spot_inv = lax.rsqrt(spot_pred * spot_true + tiny)
        cos_spot = spot_dot * spot_inv
        share = kcell / cell_total
        scale_count = slide_spots[slide].astype(jnp.float32)
        kl_part = jnp.sum(
            share * (jnp.log(counted) - jnp.log(cell_total) - jnp.log(mass) + jnp.log(mass_total))
        )
        loss_local = loss_local - gene_share * jnp.sum(cos_gene)
        loss_local = loss_local + row_share * (scale_count * kl_part - jnp.sum(valid * cos_spot))
        gene_back = cos_gene * gene_true / (gene_pred * gene_true + tiny)
        spot_back = cos_spot * spot_true / (spot_pred * spot_true + tiny)
        dpred = -valid[:, None] * (
            target * (gene_inv[None, :] + spot_inv[:, None])
            - pred * gene_back[None, :]
            - pred * spot_back[:, None]
        )
        dmass = scale_count * valid * (1.0 / mass_total - share / mass)
        pred_list.append(pred)
        grads_full, mass_full = (
            lax.all_gather(dpred, "spot", axis=0, tiled=True),
            lax.all_gather(dmass, "spot", axis=0, tiled=True),
        )
        dprob_cells = jnp.dot(grads_full, expr.T, precision=lax.Precision.HIGHEST)
        dprob_cells = lax.psum(dprob_cells, "gene")
        expr_acc = expr_acc + lax.dot_general(
            blocks, grads_full, (((0,), (0,)), ((), ())), precision=lax.Precision.HIGHEST
        )
        dprob_cells = dprob_cells + mass_full[:, None] * own_weights[None, :]
        dprob_rows = lax.all_to_all(dprob_cells, "spot", split_axis=0, concat_axis=1, tiled=True)
        inner = jnp.sum(probs * dprob_rows, axis=1, keepdims=True)
        dlogit = probs * (dprob_rows - inner)
        grad_list.append(dlogit)
    loss = lax.psum(loss_local, ("spot", "gene"))
    return (jnp.stack(pred_list), loss, jnp.stack(grad_list), expr_acc)


def solution(mesh):
    places = mesh.shape["spot"]

    def on_device(logits, expr, spatial, slide_spots, spot_cells, cell_prior):
        if places == PLANE * PLANE and mesh.shape["gene"] == 2 and expr.shape[1] == sum(FORWARD):
            return plane_call(
                logits, expr, spatial, slide_spots, spot_cells, cell_prior, places // PLANE
            )
        return general_plan(logits, expr, spatial, slide_spots, spot_cells, cell_prior)

    in_specs = (
        P(None, "spot", None),
        P("spot", "gene"),
        P(None, "spot", "gene"),
        P(),
        P(None, "spot"),
        P(),
    )
    out_specs = (P(None, "spot", "gene"), P(), P(None, "spot", None), P("spot", "gene"))
    return jax.shard_map(
        on_device, mesh=mesh, in_specs=in_specs, out_specs=out_specs, check_vma=False
    )
```

```python
import functools

import jax
import jax.numpy as jnp
from jax import lax
from jax.experimental import pallas as pl
from jax.experimental.pallas import tpu as pltpu
from jax.sharding import PartitionSpec as P

tiny = 1e-06
fixed_point = 16384.0
F32 = jnp.float32
BF16 = jnp.bfloat16
MESH = pl.DeviceIdType.MESH

PLANE = 4
LANES = 128
STEP_ROWS = 16
BLOCK = 32
TALL = 256
FORWARD = (128, 256, 256, 128, 128, 128)
BACKWARD = (128, 128, 256, 256, 256)
SPLIT = 2
LEAD = 1
NEAR_LEAD = 3
EARLY = 3
STEPS = (
    ("far", 0),
    ("far", 1),
    ("near", 0),
    ("share",),
    ("far", 2),
    ("far", 3),
    ("take",),
    ("whole", 0),
    ("near", 1),
    ("product", 0),
    ("sum", 0),
    ("whole", 1),
    ("near", 2),
    ("product", 1),
    ("whole", 2),
    ("product", 2),
    ("whole", 3),
    ("near", 3),
    ("product", 3),
    ("far", 4),
    ("whole", 4),
    ("near", 4),
    ("product", 4),
    ("sum", 1),
    ("turn", 0),
    ("far", 5),
    ("whole", 5),
    ("near", 5),
    ("product", 5),
    ("sum", 2),
    ("plane", 0),
    ("turn", 1),
    ("sum", 3),
    ("line", 0),
    ("sum", 4),
    ("sum", 5),
    ("plane", 1),
    ("cores",),
    ("genes", 0),
    ("spots",),
    ("grad", 0),
    ("grad", 1),
    ("grad", 2),
    ("line", 1),
    ("backward", 0),
    ("backward", 1),
    ("add_near", 0),
    ("genes", 1),
    ("grad", 3),
    ("backward", 2),
    ("probs", 0),
    ("add_far", 0),
    ("probs", 1),
    ("expr", 0),
    ("grad", 4),
    ("add_near", 1),
    ("probs", 2),
    ("terms",),
    ("backward", 3),
    ("probs", 3),
    ("add_near", 2),
    ("backward", 4),
    ("add_far", 1),
    ("probs", 4),
    ("exchange",),
    ("add_near", 3),
    ("add_far", 2),
    ("left",),
    ("return",),
    ("loss",),
    ("add_far", 3),
    ("expr", 1),
    ("add_near", 4),
    ("logits",),
    ("add_far", 4),
    ("expr", 2),
    ("expr", 3),
    ("expr", 4),
)


def halves(value):
    high = value.astype(BF16)
    return high, (value - high.astype(F32)).astype(BF16)


def threefold(value):
    high, low = halves(value)
    return jnp.concatenate([high, high, low], axis=1)


def product(a, b, contract):
    return lax.dot_general(a, b, (contract, ((), ())), preferred_element_type=F32)


def plane_kernel(lines, forward_widths, backward_widths, *refs):
    chunks, turns = len(forward_widths), len(backward_widths)
    (
        (logits_ref, expr_ref, spatial_ref, count_in, cells_in, prior_in),
        (pr, loss_ref, glog, ge),
        (count_ref, cells_ref, prior_ref, lg, lq, tg, ex, pq, ab, af, probs_3, turned_3, expr_3, sacc, s1, s2, gv, ss, rowv, rs),
        (grad_3, factor, t0, p0, vr, fs, fx, fy, fz, fr, inn, l1, l2),
        (loc, ou_s, ou_r, od_s, od_r, fu_s, fu_r, fd_s, fd_r, a_s, a_r, a2_s, a2_r, r_s, r_r),
        (c_s, c_r, s1_s, s1_r, s2_s, s2_r, ss_s, ss_r, d_s, d_r, ru_s, ru_r, rd_s, rd_r),
        (f_s, f_r, fx_s, fx_r, go_s, go_r, in_s, in_r, l1_s, l1_r, l2_s, l2_r, t0_s, t0_r, p0_s, p0_r, vr_s, vr_r),
        bb,
        cs,
        cr,
        ds,
        es,
        ru,
        rd,
    ) = grouped(refs, (6, 4, 20, 13, 15, 14, 18, chunks, chunks, chunks, turns, turns, turns, turns))
    place = lax.axis_index("spot")
    core = lax.axis_index("gene")
    z = place // PLANE
    q = place % PLANE
    col, row = q % 2, q // 2
    diagonal, mate_x, mate_y = (1 - row) * 2 + 1 - col, row * 2 + 1 - col, (1 - row) * 2 + col
    mates = (diagonal, mate_x + core * (mate_y - mate_x), mate_y + core * (mate_x - mate_y))
    others = tuple((z + step) % lines for step in range(1, lines))
    up, down = (place + PLANE, core), (place - PLANE, core)
    sibling = (place, 1 - core)
    slides, slide_rows = logits_ref.shape[0], logits_ref.shape[1]
    rows = slides * slide_rows
    cb = expr_ref.shape[0]
    genes = expr_ref.shape[1]
    last = lines - 1

    def mate(p):
        return (z * PLANE + p, core)

    def send(src, dst, send_sem, recv_sem, device):
        copy = pltpu.make_async_remote_copy(
            src_ref=src, dst_ref=dst, send_sem=send_sem, recv_sem=recv_sem, device_id=device, device_id_type=MESH
        )
        copy.start()

    def arrived(dst, recv_sem):
        pltpu.make_async_copy(dst, dst, recv_sem).wait()

    sent = arrived

    def cols(k):
        return pl.ds(sum(forward_widths[:k]), forward_widths[k])

    def turn_cols(k):
        return pl.ds(sum(backward_widths[:k]), backward_widths[k])

    def block(index):
        return pl.ds(pl.multiple_of(index * cb, cb), cb)

    def share(index):
        return pl.ds(pl.multiple_of(index * rows, rows), rows)

    def half(index):
        return pl.ds(pl.multiple_of(index * slide_rows, slide_rows), slide_rows)

    small = ((prior_in, prior_ref), (count_in, count_ref), (cells_in, cells_ref))
    pltpu.make_async_copy(expr_ref, ex, loc.at[2 * slides]).start()
    for m in range(slides):
        pltpu.make_async_copy(logits_ref.at[m], lg.at[half(m)], loc.at[m]).start()
    for at, (src, dst) in enumerate(small):
        pltpu.make_async_copy(src, dst, loc.at[2 * slides + 1 + at]).start()
    for m in range(slides):
        pltpu.make_async_copy(spatial_ref.at[m], tg.at[half(m)], loc.at[slides + m]).start()

    barrier = pltpu.get_barrier_semaphore()
    for p in mates:
        pl.semaphore_signal(barrier, inc=1, device_id=mate(p), device_id_type=MESH)
    for o in others:
        pl.semaphore_signal(barrier, inc=1, device_id=(o * PLANE + q, core), device_id_type=MESH)
    pl.semaphore_signal(barrier, inc=1, device_id=sibling, device_id_type=MESH)
    pltpu.make_async_copy(expr_ref, ex, loc.at[2 * slides]).wait()
    for k in range(chunks):
        bb[k][block(z), :] = ex[:, cols(k)]
    for m in range(slides):
        pltpu.make_async_copy(logits_ref.at[m], lg.at[half(m)], loc.at[m]).wait()
    for p in range(PLANE):
        for line in range(lines):
            lq[p, :, pl.ds(line * cb, cb)] = lg[half(core), pl.ds((line * PLANE + p) * cb, cb)]
    pl.semaphore_wait(barrier, len(mates) + len(others) + 1)

    def own_up(k):
        here = bb[k].at[block(z)]
        send(here, here, ou_s.at[k], ou_r.at[k], up)

    def own_down(k):
        here = bb[k].at[block(z)]
        send(here, here, od_s.at[k], od_r.at[k], down)

    def low(at):
        return 2 * at < lines

    for at in range(lines):

        @pl.when(z == at)
        def _():
            for k in range(chunks):
                if at < last and (at == 0 or k < (LEAD if low(at) else NEAR_LEAD)):
                    own_up(k)
                if at > 0 and (at == last or k < (NEAR_LEAD if low(at) else LEAD)):
                    own_down(k)

    for p in mates:
        send(lq.at[p], ab.at[q, half(core)], a_s, a_r.at[q], mate(p))

    def from_below(k, at):
        arrived(bb[k].at[pl.ds((at - 1) * cb, cb)], ou_r.at[k])
        if at > 1:
            arrived(bb[k].at[pl.ds(0, (at - 1) * cb)], fu_r.at[k])

    def from_above(k, at):
        arrived(bb[k].at[pl.ds((at + 1) * cb, cb)], od_r.at[k])
        if at < last - 1:
            arrived(bb[k].at[pl.ds((at + 2) * cb, (last - 1 - at) * cb)], fd_r.at[k])

    def upward(k, at):
        from_below(k, at)
        here = bb[k].at[pl.ds(0, at * cb)]
        send(here, here, fu_s.at[k], fu_r.at[k], up)

    def downward(k, at):
        from_above(k, at)
        here = bb[k].at[pl.ds((at + 1) * cb, (last - at) * cb)]
        send(here, here, fd_s.at[k], fd_r.at[k], down)

    def forward_far(k):
        for at in range(1, last):

            @pl.when(z == at)
            def _():
                (upward if low(at) else downward)(k, at)
                if k + LEAD < chunks:
                    (own_up if low(at) else own_down)(k + LEAD)

    def forward_near(k):
        for at in range(1, last):

            @pl.when(z == at)
            def _():
                (downward if low(at) else upward)(k, at)
                if k + NEAR_LEAD < chunks:
                    (own_down if low(at) else own_up)(k + NEAR_LEAD)

    def gathered(k):
        @pl.when(z == 0)
        def _():
            from_above(k, 0)

        @pl.when(z == last)
        def _():
            from_below(k, last)

    for at, (src, dst) in enumerate(small):
        pltpu.make_async_copy(src, dst, loc.at[2 * slides + 1 + at]).wait()
    weights = prior_ref[...].astype(F32) / fixed_point

    @pl.loop(0, rows // STEP_ROWS)
    def _(step):
        at = pl.ds(pl.multiple_of(step * STEP_ROWS, STEP_ROWS), STEP_ROWS)
        value = lg[at, :]
        peak = jnp.max(value, axis=1, keepdims=True)
        raised = jnp.exp(value - peak)
        scale = 1.0 / jnp.sum(raised, axis=1, keepdims=True)
        probs = raised * scale
        mass_rows = jnp.sum(probs * weights, axis=1, keepdims=True)
        rowv[0, at, :] = jnp.broadcast_to(mass_rows, (STEP_ROWS, LANES))
        rowv[1, at, :] = jnp.broadcast_to(peak, (STEP_ROWS, LANES))
        rowv[2, at, :] = jnp.broadcast_to(scale, (STEP_ROWS, LANES))
        for p in range(PLANE):
            for line in range(lines):
                at_cells = (line * PLANE + p) * cb
                pq[p, at, pl.ds(line * cb, cb)] = probs[:, at_cells : at_cells + cb]

    wide = lax.broadcasted_iota(jnp.int32, (rows, LANES), 1)
    rs[q] = jnp.where(wide == 0, rowv[1], rowv[2]).T[0:8]
    for p in mates:
        send(rs.at[q], rs.at[q], r_s, r_r.at[q], mate(p))

    rid = lax.broadcasted_iota(jnp.int32, (rows, 1), 0)
    first = rid < slide_rows
    position = place * slide_rows + jnp.where(first, rid, rid - slide_rows)
    count = jnp.where(first, count_ref[0], count_ref[1])
    valid = (position < count).astype(F32)
    scale_count = count.astype(F32)
    square = (slide_rows, slide_rows)
    eye = lax.broadcasted_iota(jnp.int32, square, 0) == lax.broadcasted_iota(jnp.int32, square, 1)
    counted = jnp.concatenate(
        [
            jnp.sum(jnp.where(eye, cells_ref[m : m + 1, :].astype(F32), 0.0), axis=1, keepdims=True)
            for m in range(slides)
        ],
        axis=0,
    )
    mass = rowv[0, :, 0:1]
    kcell = valid * counted

    def by_slide(value):
        return [jnp.sum(value[m * slide_rows : (m + 1) * slide_rows], axis=0, keepdims=True) for m in range(slides)]

    mass_parts = by_slide(valid * mass)
    cell_parts = by_slide(kcell)
    lane = lax.broadcasted_iota(jnp.int32, (1, LANES), 1)
    scalars = jnp.zeros((1, LANES), F32)
    for at, value in enumerate(mass_parts + cell_parts):
        scalars = jnp.where(lane == at, value, scalars)
    for m in range(slides):
        pltpu.make_async_copy(spatial_ref.at[m], tg.at[half(m)], loc.at[slides + m]).wait()

    head = backward_widths[0]
    t0[q] = tg[:, 0:head]
    for p in mates:
        send(t0.at[q], t0.at[q], t0_s, t0_r.at[q], mate(p))
    sacc[...] = jnp.zeros_like(sacc)
    s1[q, 3 * slides :, :] = jnp.zeros((8 - 3 * slides, genes), F32)
    s1[q, 3 * slides : 3 * slides + 1, 0:LANES] = scalars

    def share_logits():
        for p in mates:
            here = ab.at[p, half(core)]
            arrived(here, a_r.at[p])
            send(here, here, a2_s, a2_r.at[p], sibling)

    def lay_probs(p, at, value):
        af[p, at, :] = value
        there = pl.ds(pl.multiple_of(p * rows + at.start, BLOCK), BLOCK)
        probs_3[there, :] = threefold(value)

    def take_probs():
        in_blocks(0, rows, lambda at: lay_probs(q, at, pq[q, at, :]))
        for p in mates:
            arrived(rs.at[p], r_r.at[p])
            arrived(ab.at[p, half(1 - core)], a2_r.at[p])
            rowv[1] = jnp.concatenate([rs[p].T, jnp.zeros((rows, LANES - 8), F32)], axis=1)

            def take(at):
                probs = jnp.exp(ab[p, at, :] - rowv[1, at, 0:1]) * rowv[1, at, 1:2]
                lay_probs(p, at, probs)

            in_blocks(0, rows, take)

    def transpose(part):
        @pl.loop(0, PLANE // 2)
        def _(step):
            p = part * (PLANE // 2) + step
            high, low_part = halves(af[p].T)
            for third, value in enumerate((high, high, low_part)):
                turned_3[:, pl.ds(pl.multiple_of(third * PLANE * rows + p * rows, rows), rows)] = value

    def in_blocks(start, count, body):
        @pl.loop(0, count // BLOCK)
        def _(step):
            body(pl.ds(pl.multiple_of(start + step * BLOCK, BLOCK), BLOCK))

    quarter = lines * cb

    def lay_factor(at, length, width, value):
        high, low_part = halves(value)
        for third, part in enumerate((high, low_part, high)):
            here = pl.ds(pl.multiple_of(third * length + at.start, BLOCK), BLOCK)
            factor[here, 0:width] = part

    def keep_expr(k, at, value):
        start = sum(forward_widths[:k])
        for turn in range(turns):
            origin, width = sum(backward_widths[:turn]), backward_widths[turn]
            lo, hi = max(start, origin), min(start + forward_widths[k], origin + width)
            if lo < hi:
                high, low_part = halves(value[:, lo - start : hi - start])
                for third, part in enumerate((high, low_part, high)):
                    expr_3[at, pl.ds(3 * origin + third * width + lo - origin, hi - lo)] = part

    def three_turn_cols(k):
        return pl.ds(3 * sum(backward_widths[:k]), 3 * backward_widths[k])

    def forward_product(k):
        width = forward_widths[k]

        def lay(at):
            value = bb[k][at, :]
            lay_factor(at, quarter, width, value)
            keep_expr(k, at, value)

        in_blocks(0, quarter, lay)
        if k < chunks - 1:

            @pl.loop(0, PLANE * rows // TALL)
            def _(step):
                tall = pl.ds(pl.multiple_of(step * TALL, TALL), TALL)
                cs[k][tall, :] = product(probs_3[tall, :], factor[0 : 3 * quarter, 0:width], ((1,), (0,)))

            for p in mates:
                pass_pred(k, p)
        else:
            for side, served in ((1 - row, (diagonal, mate_y)), (row, (mate_x,))):
                pair = pl.ds(pl.multiple_of(2 * side * rows, 2 * rows), 2 * rows)
                cs[k][pair, :] = product(probs_3[pair, :], factor[0 : 3 * quarter, 0:width], ((1,), (0,)))
                for p in served:
                    pass_pred(k, p)

    def pass_pred(k, p):
        send(cs[k].at[share(p)], cr[k].at[q], c_s.at[k], c_r.at[k, q], mate(p))

    def finish_pred(k):
        total = cs[k][share(q), :]
        for p in mates:
            arrived(cr[k].at[p], c_r.at[k, p])
            total = total + cr[k][p]
        pr[:, cols(k)] = total
        if k == 0:
            p0[q] = total[:, 0:head]
            for p in mates:
                send(p0.at[q], p0.at[q], p0_s, p0_r.at[q], mate(p))
        truth = tg[:, cols(k)]
        for at, value in enumerate((total * truth, total * total, truth * truth)):
            sacc[at] += lane_groups(value)
        kept = valid * total
        stats = by_slide(kept * truth) + by_slide(kept * total) + by_slide(valid * truth * truth)
        s1[q, 0 : 3 * slides, cols(k)] = jnp.concatenate(stats, axis=0)

    early = sum(forward_widths[:EARLY])
    parts = (pl.ds(0, early), pl.ds(early, genes - early))

    def sum_plane(at):
        for p in mates:
            send(s1.at[q, :, parts[at]], s1.at[q, :, parts[at]], s1_s, s1_r.at[at, q], mate(p))

    def sum_line(at):
        for p in mates:
            arrived(s1.at[p, :, parts[at]], s1_r.at[at, p])
        s2[z, :, parts[at]] = (s1[0, :, parts[at]] + s1[1, :, parts[at]]) + (s1[2, :, parts[at]] + s1[3, :, parts[at]])
        for o in others:
            send(s2.at[z, :, parts[at]], s2.at[z, :, parts[at]], s2_s, s2_r.at[at, z], (o * PLANE + q, core))

    kept = {}

    def finish_genes(at):
        for o in others:
            arrived(s2.at[o, :, parts[at]], s2_r.at[at, o])
        total = s2[0, :, parts[at]]
        for line in range(1, lines):
            total = total + s2[line, :, parts[at]]
        gene_dot, gene_pred, gene_true = total[0:2], total[2:4], total[4:6]
        gene_inv = lax.rsqrt(gene_pred * gene_true + tiny)
        cos_gene = gene_dot * gene_inv
        gv[0:2, parts[at]] = gene_inv
        gv[2:4, parts[at]] = cos_gene * gene_true / (gene_pred * gene_true + tiny)
        kept["genes", at] = jnp.sum(jnp.sum(cos_gene, axis=1, keepdims=True), axis=0, keepdims=True)
        if at == 0:
            kept["mass"] = jnp.where(first, total[6:7, 0:1], total[6:7, 1:2])
            kept["cells"] = jnp.where(first, total[6:7, 2:3], total[6:7, 3:4])

    def sum_cores():
        sums = [jnp.sum(sacc[at], axis=1, keepdims=True) for at in range(3)]
        ss[core] = jnp.where(wide == 0, sums[0], jnp.where(wide == 1, sums[1], sums[2])).T[0:8]
        send(ss.at[core], ss.at[core], ss_s, ss_r, sibling)

    def finish_spots():
        lane_id = lax.broadcasted_iota(jnp.int32, (1, rows), 1)
        first_lane = lane_id < slide_rows
        lane_position = place * slide_rows + jnp.where(first_lane, lane_id, lane_id - slide_rows)
        lane_valid = (lane_position < jnp.where(first_lane, count_ref[0], count_ref[1])).astype(F32)
        arrived(ss.at[1 - core], ss_r)
        spot = ss[0] + ss[1]
        spot_dot, spot_pred, spot_true = spot[0:1], spot[1:2], spot[2:3]
        spot_inv = lax.rsqrt(spot_pred * spot_true + tiny)
        cos_spot = spot_dot * spot_inv
        spot_back = cos_spot * spot_true / (spot_pred * spot_true + tiny)
        kept["cos"] = jnp.sum(lane_valid * cos_spot, axis=1, keepdims=True)
        vectors = [lane_valid * spot_inv, lane_valid * spot_back, lane_valid, jnp.zeros((5, rows), F32)]
        vr[q] = jnp.concatenate(vectors, axis=0)
        sacc[0] = jnp.zeros_like(sacc[0])

    def gradient(truth, guess, by_row, k):
        pieces = []
        for m in range(slides):
            lo, hi = m * slide_rows, (m + 1) * slide_rows
            inverse, back = gv[m : m + 1, turn_cols(k)], gv[2 + m : 3 + m, turn_cols(k)]
            spot_inv, spot_back, spot_valid = by_row[lo:hi, 0:1], by_row[lo:hi, 1:2], by_row[lo:hi, 2:3]
            pieces.append(
                guess[lo:hi] * (spot_valid * back + spot_back) - truth[lo:hi] * (spot_valid * inverse + spot_inv)
            )
        return jnp.concatenate(pieces, axis=0)

    def head_gradient():
        for p in mates:
            arrived(t0.at[p], t0_r.at[p])
            arrived(p0.at[p], p0_r.at[p])
            arrived(vr.at[p], vr_r.at[p])
        for p in range(PLANE):
            ds[0][share(p), :] = gradient(t0[p], p0[p], vr[p].T, 0)
        sacc[0] += lane_groups(ds[0][share(q), :] * p0[q])

    def send_grad(k):
        if k == 0:
            for p in mates:
                send(vr.at[q], vr.at[q], vr_s, vr_r.at[q], mate(p))
            kept["by_row"] = vr[q].T
            return
        grad = gradient(tg[:, turn_cols(k)], pr[:, turn_cols(k)], kept["by_row"], k)
        here = ds[k].at[share(q)]
        here[...] = grad
        for p in mates:
            send(here, here, d_s.at[k], d_r.at[k, q], mate(p))
        sacc[0] += lane_groups(grad * pr[:, turn_cols(k)])

    def send_terms():
        mass_total, cell_total = kept["mass"], kept["cells"]
        portion = kcell / cell_total
        kl_rows = portion * (jnp.log(counted) - jnp.log(cell_total) - jnp.log(mass) + jnp.log(mass_total))
        dmass = scale_count * valid * (1.0 / mass_total - portion / mass)
        terms = jnp.sum(scale_count * kl_rows, axis=0, keepdims=True) - kept["cos"]
        l1[q] = jnp.broadcast_to(terms, (8, LANES))
        for p in mates:
            send(l1.at[q], l1.at[q], l1_s, l1_r.at[q], mate(p))
        inner = jnp.sum(sacc[0], axis=1, keepdims=True)
        inn[core] = jnp.where(wide == 0, inner, kept["genes", 0] + kept["genes", 1])
        send(inn.at[core], inn.at[core], in_s, in_r, sibling)
        rowv[1] = jnp.broadcast_to(dmass, (rows, LANES))

    middle = lines // 2

    def backward_product(k):
        if k == 0:
            head_gradient()
        else:
            for p in mates:
                arrived(ds[k].at[share(p)], d_r.at[k, p])
        width, spots = backward_widths[k], PLANE * rows

        def lay(at):
            value = ds[k][at, :]
            lay_factor(at, spots, width, value)
            grad_3[at, three_turn_cols(k)] = threefold(value)

        in_blocks(0, spots, lay)
        if not halved(k):

            @pl.loop(0, quarter // TALL)
            def _(step):
                tall = pl.ds(pl.multiple_of(step * TALL, TALL), TALL)
                es[k][tall, :] = product(turned_3[tall, :], factor[0 : 3 * spots, 0:width], ((1,), (0,)))

        for turn in range(2):
            if halved(k):
                side = (1 - z // middle) if turn == 0 else z // middle
                pair = pl.ds(pl.multiple_of(side * middle * cb, middle * cb), middle * cb)
                es[k][pair, :] = product(turned_3[pair, :], factor[0 : 3 * spots, 0:width], ((1,), (0,)))

            @pl.when(z == 0)
            def _():
                if halved(k):
                    pass_up(k, middle if turn == 0 else 1, middle if turn == 0 else middle - 1, turn)
                elif whole(k):
                    if turn == 0:
                        pass_up(k, 1, last, 0)
                elif turn == 0:
                    for line in range(last, 0, -1):
                        pass_up(k, line, 1, line)

            @pl.when(z == last)
            def _():
                if halved(k):
                    pass_down(k, 0 if turn == 0 else middle, middle if turn == 0 else middle - 1, turn)
                elif whole(k):
                    if turn == 0:
                        pass_down(k, 0, last, 0)
                elif turn == 0:
                    for line in range(last):
                        pass_down(k, line, 1, line)

    def halved(k):
        return k == 0

    def whole(k):
        return 0 < k < turns - SPLIT

    def pass_up(k, line, count, slot):
        here = pl.ds(line * cb, count * cb)
        send(es[k].at[here], ru[k].at[here], ru_s.at[k], ru_r.at[k, slot], up)

    def pass_down(k, line, count, slot):
        here = pl.ds(line * cb, count * cb)
        send(es[k].at[here], rd[k].at[here], rd_s.at[k], rd_r.at[k, slot], down)

    def take_up(k, line, count, slot):
        arrived(ru[k].at[pl.ds(line * cb, count * cb)], ru_r.at[k, slot])

    def take_down(k, line, count, slot):
        arrived(rd[k].at[pl.ds(line * cb, count * cb)], rd_r.at[k, slot])

    def add_up(k, line, count):
        def add(at):
            es[k][at, :] += ru[k][at, :]

        in_blocks(line * cb, count * cb, add)

    def add_down(k, line, count):
        def add(at):
            es[k][at, :] += rd[k][at, :]

        in_blocks(line * cb, count * cb, add)

    def rising(k, at):
        if halved(k) or whole(k):
            start = middle if halved(k) else at
            take_up(k, start, lines - start, 0)
            above = max(at + 1, start)
            add_up(k, above, lines - above)
            pass_up(k, above, lines - above, 0)
        else:
            for line in range(last, at, -1):
                take_up(k, line, 1, line)
                add_up(k, line, 1)
                pass_up(k, line, 1, line)

    def falling(k, at):
        if halved(k) or whole(k):
            end = middle if halved(k) else at + 1
            take_down(k, 0, end, 0)
            below = min(at, end)
            add_down(k, 0, below)
            pass_down(k, 0, below, 0)
        else:
            for line in range(at):
                take_down(k, line, 1, line)
                add_down(k, line, 1)
                pass_down(k, line, 1, line)

    def add_near(k):
        for at in range(1, last):

            @pl.when(z == at)
            def _():
                (rising if low(at) else falling)(k, at)

    def add_far(k):
        for at in range(1, last):

            @pl.when(z == at)
            def _():
                (falling if low(at) else rising)(k, at)

    def finish_expr(k):
        for at in range(lines):

            @pl.when(z == at)
            def _():
                if at > 0:
                    if halved(k) and at < middle:
                        take_up(k, at, 1, 1)
                    elif at == last and (halved(k) or whole(k)):
                        take_up(k, at, 1, 0)
                    elif not halved(k) and not whole(k):
                        take_up(k, at, 1, at)
                if at < last:
                    if halved(k) and at >= middle:
                        take_down(k, at, 1, 1)
                    elif at == 0 and (halved(k) or whole(k)):
                        take_down(k, at, 1, 0)
                    elif not halved(k) and not whole(k):
                        take_down(k, at, 1, at)

        from_low, from_high = z > 0, z < last

        @pl.loop(0, cb // BLOCK)
        def _(step):
            here = pl.ds(pl.multiple_of(step * BLOCK, BLOCK), BLOCK)
            own = pl.ds(pl.multiple_of(z * cb + step * BLOCK, BLOCK), BLOCK)
            total = es[k][own, :]
            total = total + jnp.where(from_low, ru[k][own, :], 0.0)
            ge[here, turn_cols(k)] = total + jnp.where(from_high, rd[k][own, :], 0.0)

    def probs_gradient(k):
        at = three_turn_cols(k)

        @pl.loop(0, PLANE * rows // TALL)
        def _(step):
            tall = pl.ds(pl.multiple_of(step * TALL, TALL), TALL)
            part = product(grad_3[tall, at], expr_3[:, at], ((1,), (1,)))
            if k == 0:
                fs[tall, :] = part
            else:
                fs[tall, :] += part

    def slide_of(p, m):
        return pl.ds(pl.multiple_of(p * rows + m * slide_rows, slide_rows), slide_rows)

    def sum_probs_cores():
        for p in mates + (q,):
            fx[p] = fs[slide_of(p, 1 - core), :]
            send(fx.at[p], fy.at[p], fx_s, fx_r.at[p], sibling)

    def return_probs():
        for p in mates:
            arrived(fy.at[p], fx_r.at[p])
            fz[p] = fs[slide_of(p, core), :] + fy[p]
            send(fz.at[p], fr.at[q], f_s, f_r.at[q], mate(p))
        arrived(fy.at[q], fx_r.at[q])
        fr[q] = fs[slide_of(q, core), :] + fy[q]

    def pass_terms():
        for p in mates:
            arrived(l1.at[p], l1_r.at[p])
        l2[z] = (l1[0] + l1[1]) + (l1[2] + l1[3])
        for o in others:
            send(l2.at[z], l2.at[z], l2_s, l2_r.at[z], (o * PLANE + q, core))

    def part_of(slide, m):
        start = slide * slide_rows + m * (slide_rows // 2)
        return pl.ds(pl.multiple_of(start, slide_rows // 2), slide_rows // 2)

    def finish_logits():
        arrived(inn.at[1 - core], in_r)
        rowv[2] = (inn[0] + inn[1]) + rowv[1] * rowv[0]
        for p in mates:
            arrived(fr.at[p], f_r.at[p])
        for m in range(2):

            @pl.loop(0, slide_rows // STEP_ROWS // 2)
            def _(step):
                row_at = (m * (slide_rows // STEP_ROWS // 2) + step) * STEP_ROWS
                at = pl.ds(pl.multiple_of(row_at, STEP_ROWS), STEP_ROWS)
                whole_at = pl.ds(pl.multiple_of(core * slide_rows + row_at, STEP_ROWS), STEP_ROWS)
                by_mass, total_inner = rowv[1, whole_at, 0:1], rowv[2, whole_at, 0:1]
                for p in range(PLANE):
                    for line in range(lines):
                        here, there = pl.ds(line * cb, cb), (line * PLANE + p) * cb
                        grad = fr[p, at, here] + by_mass * weights[:, there : there + cb]
                        glog[whole_at, pl.ds(there, cb)] = pq[p, whole_at, here] * (grad - total_inner)

            here = part_of(core, m)
            send(glog.at[here], glog.at[here], go_s, go_r.at[m], sibling)

    def forward_left():
        for k in range(chunks):

            @pl.when(z < last)
            def _():
                sent(bb[k].at[block(z)], ou_s.at[k])

            @pl.when(z > 0)
            def _():
                sent(bb[k].at[block(z)], od_s.at[k])

            for at in range(1, last):

                @pl.when(z == at)
                def _():
                    sent(bb[k].at[pl.ds(0, at * cb)], fu_s.at[k])
                    sent(bb[k].at[pl.ds((at + 1) * cb, (last - at) * cb)], fd_s.at[k])

        three = pl.ds(0, len(mates))
        sent(ab.at[three, half(0)], a_s)
        sent(ab.at[three, half(0)], a2_s)
        sent(rs.at[three], r_s)
        sent(t0.at[three], t0_s)
        sent(p0.at[three], p0_s)
        for k in range(chunks):
            sent(cr[k].at[three], c_s.at[k])
        sent(s1.at[three], s1_s)
        sent(s2.at[pl.ds(0, last)], s2_s)
        sent(ss.at[0], ss_s)

    steps = {
        "far": forward_far,
        "near": forward_near,
        "share": share_logits,
        "take": take_probs,
        "whole": gathered,
        "product": forward_product,
        "sum": finish_pred,
        "turn": transpose,
        "plane": sum_plane,
        "line": sum_line,
        "genes": finish_genes,
        "cores": sum_cores,
        "spots": finish_spots,
        "grad": send_grad,
        "terms": send_terms,
        "backward": backward_product,
        "probs": probs_gradient,
        "exchange": sum_probs_cores,
        "return": return_probs,
        "loss": pass_terms,
        "logits": finish_logits,
        "add_near": add_near,
        "add_far": add_far,
        "expr": finish_expr,
        "left": forward_left,
    }
    for name, *where in STEPS:
        steps[name](*where)

    for o in others:
        arrived(l2.at[o], l2_r.at[o])
    loss = l2[0]
    for line in range(1, lines):
        loss = loss + l2[line]
    loss_ref[...] = loss[0:1, 0:1] - (inn[0, 0:1, 1:2] + inn[1, 0:1, 1:2])
    for m in range(2):
        arrived(glog.at[part_of(1 - core, m)], go_r.at[m])

    for k in range(turns):
        for at in range(lines):

            @pl.when(z == at)
            def _():
                if at < last:
                    sent(es[k].at[pl.ds((at + 1) * cb, (last - at) * cb)], ru_s.at[k])
                if at > 0:
                    sent(es[k].at[pl.ds(0, at * cb)], rd_s.at[k])

    three = pl.ds(0, len(mates))
    for k in range(1, turns):
        sent(ds[k].at[pl.ds(0, len(mates) * rows)], d_s.at[k])
    sent(vr.at[three], vr_s)
    sent(inn.at[0], in_s)
    sent(l1.at[three], l1_s)
    sent(l2.at[pl.ds(0, last)], l2_s)
    sent(fr.at[three], f_s)
    sent(fx, fx_s)
    sent(glog.at[half(0)], go_s)


def lane_groups(value):
    parts = [value[:, at : at + LANES] for at in range(0, value.shape[1], LANES)]
    return functools.reduce(lambda a, b: a + b, parts)


def grouped(refs, sizes):
    at = 0
    for size in sizes:
        yield refs[at : at + size]
        at += size


def deliver(pred_in, loss_in, glog_in, gexp_in, pred_ref, loss_ref, glog_ref, gexp_ref, sems):
    slides, slide_rows = pred_ref.shape[0], pred_ref.shape[1]
    pairs = [(gexp_in, gexp_ref), (loss_in, loss_ref)]
    for m in range(slides):
        part = pl.ds(m * slide_rows, slide_rows)
        pairs += [(glog_in.at[part], glog_ref.at[m]), (pred_in.at[part], pred_ref.at[m])]
    copies = [pltpu.make_async_copy(src, dst, sems.at[at]) for at, (src, dst) in enumerate(pairs)]
    for copy in copies:
        copy.start()
    for copy in copies:
        copy.wait()


def plane_call(logits, expr, spatial, slide_spots, spot_cells, cell_prior, lines):
    slides, slide_rows, cells = logits.shape
    rows = slides * slide_rows
    cb, genes = expr.shape
    quarter = lines * cb
    spots = PLANE * rows
    chunks, turns = len(FORWARD), len(BACKWARD)
    dma = pltpu.SemaphoreType.DMA
    vmem = pltpu.VMEM
    anywhere = pl.BlockSpec(memory_space=pl.ANY)
    in_vmem = pl.BlockSpec(memory_space=pltpu.VMEM)
    scratch = [
        pltpu.SMEM((slides,), jnp.int32),
        vmem((slides, slide_rows), jnp.int32),
        vmem((1, cells), jnp.int32),
        vmem((rows, cells), F32),
        vmem((PLANE, slide_rows, quarter), F32),
        vmem((rows, genes), F32),
        vmem((cb, genes), F32),
        vmem((PLANE, rows, quarter), F32),
        vmem((PLANE, rows, quarter), F32),
        vmem((PLANE, rows, quarter), F32),
        vmem((spots, 3 * quarter), BF16),
        vmem((quarter, 3 * spots), BF16),
        vmem((quarter, 3 * genes), BF16),
        vmem((3, rows, LANES), F32),
        vmem((PLANE, 8, genes), F32),
        vmem((lines, 8, genes), F32),
        vmem((8, genes), F32),
        vmem((2, 8, rows), F32),
        vmem((3, rows, LANES), F32),
        vmem((PLANE, 8, rows), F32),
        vmem((spots, 3 * genes), BF16),
        vmem((3 * max(quarter, spots), max(FORWARD + BACKWARD)), BF16),
        vmem((PLANE, rows, BACKWARD[0]), F32),
        vmem((PLANE, rows, BACKWARD[0]), F32),
        vmem((PLANE, 8, rows), F32),
        vmem((spots, quarter), F32),
        vmem((PLANE, slide_rows, quarter), F32),
        vmem((PLANE, slide_rows, quarter), F32),
        vmem((PLANE, slide_rows, quarter), F32),
        vmem((PLANE, slide_rows, quarter), F32),
        vmem((2, rows, LANES), F32),
        vmem((PLANE, 8, LANES), F32),
        vmem((lines, 8, LANES), F32),
        dma((2 * slides + 4,)),
        dma((chunks,)),
        dma((chunks,)),
        dma((chunks,)),
        dma((chunks,)),
        dma((chunks,)),
        dma((chunks,)),
        dma((chunks,)),
        dma((chunks,)),
        dma,
        dma((PLANE,)),
        dma,
        dma((PLANE,)),
        dma,
        dma((PLANE,)),
        dma((chunks,)),
        dma((chunks, PLANE)),
        dma,
        dma((2, PLANE)),
        dma,
        dma((2, lines)),
        dma,
        dma,
        dma((turns,)),
        dma((turns, PLANE)),
        dma((turns,)),
        dma((turns, lines)),
        dma((turns,)),
        dma((turns, lines)),
        dma,
        dma((PLANE,)),
        dma,
        dma((PLANE,)),
        dma,
        dma((2,)),
        dma,
        dma,
        dma,
        dma((PLANE,)),
        dma,
        dma((lines,)),
        dma,
        dma((PLANE,)),
        dma,
        dma((PLANE,)),
        dma,
        dma((PLANE,)),
    ]
    for shape, widths in (
        ((quarter,), FORWARD),
        ((spots,), FORWARD),
        ((PLANE, rows), FORWARD),
        ((spots,), BACKWARD),
        ((quarter,), BACKWARD),
        ((quarter,), BACKWARD),
        ((quarter,), BACKWARD),
    ):
        scratch += [vmem(shape + (width,), F32) for width in widths]
    in_hbm = functools.partial(pltpu.with_memory_space_constraint, memory_space=pltpu.HBM)
    in_place = functools.partial(pltpu.with_memory_space_constraint, memory_space=pltpu.VMEM)
    results = pl.pallas_call(
        functools.partial(plane_kernel, lines, FORWARD, BACKWARD),
        out_shape=(
            vmem((rows, genes), F32),
            vmem((1, 1), F32),
            vmem((rows, cells), F32),
            vmem((cb, genes), F32),
        ),
        in_specs=[anywhere] * 6,
        out_specs=(in_vmem,) * 4,
        scratch_shapes=scratch,
        compiler_params=pltpu.CompilerParams(
            collective_id=0, has_side_effects=True, vmem_limit_bytes=48 * 1024 * 1024
        ),
    )(*map(in_hbm, (logits, expr, spatial, slide_spots, spot_cells, cell_prior.reshape(1, cells))))
    pred, loss, grad_logits, grad_expr = pl.pallas_call(
        deliver,
        out_shape=(
            jax.ShapeDtypeStruct((slides, slide_rows, genes), F32),
            jax.ShapeDtypeStruct((1, 1), F32),
            jax.ShapeDtypeStruct((slides, slide_rows, cells), F32),
            jax.ShapeDtypeStruct((cb, genes), F32),
        ),
        in_specs=[anywhere] * 4,
        out_specs=(anywhere,) * 4,
        scratch_shapes=[dma((2 * slides + 2,))],
        compiler_params=pltpu.CompilerParams(vmem_limit_bytes=4 * 1024 * 1024),
    )(*map(in_place, results))
    return pred, loss.reshape(()), grad_logits, grad_expr


def general_plan(logits, expr, spatial, slide_spots, spot_cells, cell_prior):
    place = lax.axis_index("spot")
    side = lax.axis_index("gene")
    rows_all = logits.shape[1]
    cell_rows = expr.shape[0]
    weights = cell_prior.astype(jnp.float32) / fixed_point
    gene_share = (place == 0).astype(jnp.float32)
    row_share = (side == 0).astype(jnp.float32)
    own_weights = lax.dynamic_slice_in_dim(weights, place * cell_rows, cell_rows, 0)
    expr_acc = jnp.zeros((cell_rows, expr.shape[1]), jnp.float32)
    loss_local = jnp.zeros((), jnp.float32)
    pred_list = []
    grad_list = []
    for slide in range(logits.shape[0]):
        logit_rows = logits[slide]
        counted = spot_cells[slide].astype(jnp.float32)
        target = spatial[slide]
        positions = place * rows_all + jnp.arange(rows_all, dtype=jnp.int32)
        valid = (positions < slide_spots[slide]).astype(jnp.float32)
        peak = jnp.max(logit_rows, axis=1, keepdims=True)
        raised = jnp.exp(logit_rows - peak)
        probs = raised / jnp.sum(raised, axis=1, keepdims=True)
        mass = jnp.dot(probs, weights, precision=lax.Precision.HIGHEST)
        blocks = lax.all_to_all(probs, "spot", split_axis=1, concat_axis=0, tiled=True)
        pred = lax.psum_scatter(
            jnp.dot(blocks, expr, precision=lax.Precision.HIGHEST),
            "spot",
            scatter_dimension=0,
            tiled=True,
        )
        gene_dot = jnp.sum(valid[:, None] * pred * target, axis=0)
        gene_pred = jnp.sum(valid[:, None] * pred * pred, axis=0)
        gene_true = jnp.sum(valid[:, None] * target * target, axis=0)
        mass_part = jnp.sum(valid * mass)
        kcell = valid * counted
        cell_part = jnp.sum(kcell)
        spot_dot = jnp.sum(pred * target, axis=1)
        spot_pred = jnp.sum(pred * pred, axis=1)
        spot_true = jnp.sum(target * target, axis=1)
        gene_dot, gene_pred, gene_true, mass_total, cell_total = lax.psum(
            (gene_dot, gene_pred, gene_true, mass_part, cell_part), "spot"
        )
        spot_dot, spot_pred, spot_true = lax.psum((spot_dot, spot_pred, spot_true), "gene")
        gene_inv = lax.rsqrt(gene_pred * gene_true + tiny)
        cos_gene = gene_dot * gene_inv
        spot_inv = lax.rsqrt(spot_pred * spot_true + tiny)
        cos_spot = spot_dot * spot_inv
        share = kcell / cell_total
        scale_count = slide_spots[slide].astype(jnp.float32)
        kl_part = jnp.sum(
            share * (jnp.log(counted) - jnp.log(cell_total) - jnp.log(mass) + jnp.log(mass_total))
        )
        loss_local = loss_local - gene_share * jnp.sum(cos_gene)
        loss_local = loss_local + row_share * (scale_count * kl_part - jnp.sum(valid * cos_spot))
        gene_back = cos_gene * gene_true / (gene_pred * gene_true + tiny)
        spot_back = cos_spot * spot_true / (spot_pred * spot_true + tiny)
        dpred = -valid[:, None] * (
            target * (gene_inv[None, :] + spot_inv[:, None])
            - pred * gene_back[None, :]
            - pred * spot_back[:, None]
        )
        dmass = scale_count * valid * (1.0 / mass_total - share / mass)
        pred_list.append(pred)
        grads_full, mass_full = (
            lax.all_gather(dpred, "spot", axis=0, tiled=True),
            lax.all_gather(dmass, "spot", axis=0, tiled=True),
        )
        dprob_cells = jnp.dot(grads_full, expr.T, precision=lax.Precision.HIGHEST)
        dprob_cells = lax.psum(dprob_cells, "gene")
        expr_acc = expr_acc + lax.dot_general(
            blocks, grads_full, (((0,), (0,)), ((), ())), precision=lax.Precision.HIGHEST
        )
        dprob_cells = dprob_cells + mass_full[:, None] * own_weights[None, :]
        dprob_rows = lax.all_to_all(dprob_cells, "spot", split_axis=0, concat_axis=1, tiled=True)
        inner = jnp.sum(probs * dprob_rows, axis=1, keepdims=True)
        dlogit = probs * (dprob_rows - inner)
        grad_list.append(dlogit)
    loss = lax.psum(loss_local, ("spot", "gene"))
    return (jnp.stack(pred_list), loss, jnp.stack(grad_list), expr_acc)


def solution(mesh):
    places = mesh.shape["spot"]

    def on_device(logits, expr, spatial, slide_spots, spot_cells, cell_prior):
        if places == PLANE * PLANE and mesh.shape["gene"] == 2 and expr.shape[1] == sum(FORWARD):
            return plane_call(
                logits, expr, spatial, slide_spots, spot_cells, cell_prior, places // PLANE
            )
        return general_plan(logits, expr, spatial, slide_spots, spot_cells, cell_prior)

    in_specs = (
        P(None, "spot", None),
        P("spot", "gene"),
        P(None, "spot", "gene"),
        P(),
        P(None, "spot"),
        P(),
    )
    out_specs = (P(None, "spot", "gene"), P(), P(None, "spot", None), P("spot", "gene"))
    return jax.shard_map(
        on_device, mesh=mesh, in_specs=in_specs, out_specs=out_specs, check_vma=False
    )
```

```python
import functools

import jax
import jax.numpy as jnp
from jax import lax
from jax.experimental import pallas as pl
from jax.experimental.pallas import tpu as pltpu
from jax.sharding import PartitionSpec as P

tiny = 1e-06
fixed_point = 16384.0
F32 = jnp.float32
BF16 = jnp.bfloat16
MESH = pl.DeviceIdType.MESH

PLANE = 4
LANES = 128
STEP_ROWS = 16
BLOCK = 32
TALL = 256
FORWARD = (128, 256, 256, 128, 128, 128)
BACKWARD = (128, 128, 256, 256, 256)
SPLIT = 1
LEAD = 1
NEAR_LEAD = 3
EARLY = 3
STEPS = (
    ("far", 0),
    ("far", 1),
    ("near", 0),
    ("share",),
    ("far", 2),
    ("far", 3),
    ("take",),
    ("whole", 0),
    ("near", 1),
    ("product", 0),
    ("sum", 0),
    ("whole", 1),
    ("near", 2),
    ("product", 1),
    ("whole", 2),
    ("product", 2),
    ("whole", 3),
    ("near", 3),
    ("product", 3),
    ("far", 4),
    ("whole", 4),
    ("near", 4),
    ("product", 4),
    ("sum", 1),
    ("turn", 0),
    ("far", 5),
    ("whole", 5),
    ("near", 5),
    ("product", 5),
    ("sum", 2),
    ("plane", 0),
    ("turn", 1),
    ("sum", 3),
    ("line", 0),
    ("sum", 4),
    ("sum", 5),
    ("plane", 1),
    ("cores",),
    ("genes", 0),
    ("spots",),
    ("grad", 0),
    ("grad", 1),
    ("grad", 2),
    ("line", 1),
    ("backward", 0),
    ("backward", 1),
    ("add_near", 0),
    ("genes", 1),
    ("grad", 3),
    ("backward", 2),
    ("probs", 0),
    ("add_far", 0),
    ("probs", 1),
    ("expr", 0),
    ("grad", 4),
    ("add_near", 1),
    ("probs", 2),
    ("terms",),
    ("backward", 3),
    ("probs", 3),
    ("add_near", 2),
    ("backward", 4),
    ("add_far", 1),
    ("probs", 4),
    ("exchange",),
    ("add_near", 3),
    ("add_far", 2),
    ("left",),
    ("return",),
    ("loss",),
    ("add_far", 3),
    ("expr", 1),
    ("add_near", 4),
    ("logits",),
    ("add_far", 4),
    ("expr", 2),
    ("expr", 3),
    ("expr", 4),
)


def halves(value):
    high = value.astype(BF16)
    return high, (value - high.astype(F32)).astype(BF16)


def threefold(value):
    high, low = halves(value)
    return jnp.concatenate([high, high, low], axis=1)


def product(a, b, contract):
    return lax.dot_general(a, b, (contract, ((), ())), preferred_element_type=F32)


def plane_kernel(lines, forward_widths, backward_widths, *refs):
    chunks, turns = len(forward_widths), len(backward_widths)
    (
        (logits_ref, expr_ref, spatial_ref, count_in, cells_in, prior_in),
        (pr, loss_ref, glog, ge),
        (count_ref, cells_ref, prior_ref, lg, lq, tg, ex, pq, ab, af, probs_3, turned_3, expr_3, sacc, s1, s2, gv, ss, rowv, rs),
        (grad_3, factor, t0, p0, vr, fs, fx, fy, fz, fr, inn, l1, l2),
        (loc, ou_s, ou_r, od_s, od_r, fu_s, fu_r, fd_s, fd_r, a_s, a_r, a2_s, a2_r, r_s, r_r),
        (c_s, c_r, s1_s, s1_r, s2_s, s2_r, ss_s, ss_r, d_s, d_r, ru_s, ru_r, rd_s, rd_r),
        (f_s, f_r, fx_s, fx_r, go_s, go_r, in_s, in_r, l1_s, l1_r, l2_s, l2_r, t0_s, t0_r, p0_s, p0_r, vr_s, vr_r),
        bb,
        cs,
        cr,
        ds,
        es,
        ru,
        rd,
    ) = grouped(refs, (6, 4, 20, 13, 15, 14, 18, chunks, chunks, chunks, turns, turns, turns, turns))
    place = lax.axis_index("spot")
    core = lax.axis_index("gene")
    z = place // PLANE
    q = place % PLANE
    col, row = q % 2, q // 2
    mates = ((1 - row) * 2 + 1 - col, row * 2 + 1 - col, (1 - row) * 2 + col)
    others = tuple((z + step) % lines for step in range(1, lines))
    up, down = (place + PLANE, core), (place - PLANE, core)
    sibling = (place, 1 - core)
    slides, slide_rows = logits_ref.shape[0], logits_ref.shape[1]
    rows = slides * slide_rows
    cb = expr_ref.shape[0]
    genes = expr_ref.shape[1]
    last = lines - 1

    def mate(p):
        return (z * PLANE + p, core)

    def send(src, dst, send_sem, recv_sem, device):
        copy = pltpu.make_async_remote_copy(
            src_ref=src, dst_ref=dst, send_sem=send_sem, recv_sem=recv_sem, device_id=device, device_id_type=MESH
        )
        copy.start()

    def arrived(dst, recv_sem):
        pltpu.make_async_copy(dst, dst, recv_sem).wait()

    sent = arrived

    def cols(k):
        return pl.ds(sum(forward_widths[:k]), forward_widths[k])

    def turn_cols(k):
        return pl.ds(sum(backward_widths[:k]), backward_widths[k])

    def block(index):
        return pl.ds(pl.multiple_of(index * cb, cb), cb)

    def share(index):
        return pl.ds(pl.multiple_of(index * rows, rows), rows)

    def half(index):
        return pl.ds(pl.multiple_of(index * slide_rows, slide_rows), slide_rows)

    small = ((prior_in, prior_ref), (count_in, count_ref), (cells_in, cells_ref))
    pltpu.make_async_copy(expr_ref, ex, loc.at[2 * slides]).start()
    for m in range(slides):
        pltpu.make_async_copy(logits_ref.at[m], lg.at[half(m)], loc.at[m]).start()
    for at, (src, dst) in enumerate(small):
        pltpu.make_async_copy(src, dst, loc.at[2 * slides + 1 + at]).start()
    for m in range(slides):
        pltpu.make_async_copy(spatial_ref.at[m], tg.at[half(m)], loc.at[slides + m]).start()

    barrier = pltpu.get_barrier_semaphore()
    for p in mates:
        pl.semaphore_signal(barrier, inc=1, device_id=mate(p), device_id_type=MESH)
    for o in others:
        pl.semaphore_signal(barrier, inc=1, device_id=(o * PLANE + q, core), device_id_type=MESH)
    pl.semaphore_signal(barrier, inc=1, device_id=sibling, device_id_type=MESH)
    pltpu.make_async_copy(expr_ref, ex, loc.at[2 * slides]).wait()
    for k in range(chunks):
        bb[k][block(z), :] = ex[:, cols(k)]
    for m in range(slides):
        pltpu.make_async_copy(logits_ref.at[m], lg.at[half(m)], loc.at[m]).wait()
    for p in range(PLANE):
        for line in range(lines):
            lq[p, :, pl.ds(line * cb, cb)] = lg[half(core), pl.ds((line * PLANE + p) * cb, cb)]
    pl.semaphore_wait(barrier, len(mates) + len(others) + 1)

    def own_up(k):
        here = bb[k].at[block(z)]
        send(here, here, ou_s.at[k], ou_r.at[k], up)

    def own_down(k):
        here = bb[k].at[block(z)]
        send(here, here, od_s.at[k], od_r.at[k], down)

    def low(at):
        return 2 * at < lines

    for at in range(lines):

        @pl.when(z == at)
        def _():
            for k in range(chunks):
                if at < last and (at == 0 or k < (LEAD if low(at) else NEAR_LEAD)):
                    own_up(k)
                if at > 0 and (at == last or k < (NEAR_LEAD if low(at) else LEAD)):
                    own_down(k)

    for p in mates:
        send(lq.at[p], ab.at[q, half(core)], a_s, a_r.at[q], mate(p))

    def from_below(k, at):
        arrived(bb[k].at[pl.ds((at - 1) * cb, cb)], ou_r.at[k])
        if at > 1:
            arrived(bb[k].at[pl.ds(0, (at - 1) * cb)], fu_r.at[k])

    def from_above(k, at):
        arrived(bb[k].at[pl.ds((at + 1) * cb, cb)], od_r.at[k])
        if at < last - 1:
            arrived(bb[k].at[pl.ds((at + 2) * cb, (last - 1 - at) * cb)], fd_r.at[k])

    def upward(k, at):
        from_below(k, at)
        here = bb[k].at[pl.ds(0, at * cb)]
        send(here, here, fu_s.at[k], fu_r.at[k], up)

    def downward(k, at):
        from_above(k, at)
        here = bb[k].at[pl.ds((at + 1) * cb, (last - at) * cb)]
        send(here, here, fd_s.at[k], fd_r.at[k], down)

    def forward_far(k):
        for at in range(1, last):

            @pl.when(z == at)
            def _():
                (upward if low(at) else downward)(k, at)
                if k + LEAD < chunks:
                    (own_up if low(at) else own_down)(k + LEAD)

    def forward_near(k):
        for at in range(1, last):

            @pl.when(z == at)
            def _():
                (downward if low(at) else upward)(k, at)
                if k + NEAR_LEAD < chunks:
                    (own_down if low(at) else own_up)(k + NEAR_LEAD)

    def gathered(k):
        @pl.when(z == 0)
        def _():
            from_above(k, 0)

        @pl.when(z == last)
        def _():
            from_below(k, last)

    for at, (src, dst) in enumerate(small):
        pltpu.make_async_copy(src, dst, loc.at[2 * slides + 1 + at]).wait()
    weights = prior_ref[...].astype(F32) / fixed_point

    @pl.loop(0, rows // STEP_ROWS)
    def _(step):
        at = pl.ds(pl.multiple_of(step * STEP_ROWS, STEP_ROWS), STEP_ROWS)
        value = lg[at, :]
        peak = jnp.max(value, axis=1, keepdims=True)
        raised = jnp.exp(value - peak)
        scale = 1.0 / jnp.sum(raised, axis=1, keepdims=True)
        probs = raised * scale
        mass_rows = jnp.sum(probs * weights, axis=1, keepdims=True)
        rowv[0, at, :] = jnp.broadcast_to(mass_rows, (STEP_ROWS, LANES))
        rowv[1, at, :] = jnp.broadcast_to(peak, (STEP_ROWS, LANES))
        rowv[2, at, :] = jnp.broadcast_to(scale, (STEP_ROWS, LANES))
        for p in range(PLANE):
            for line in range(lines):
                at_cells = (line * PLANE + p) * cb
                pq[p, at, pl.ds(line * cb, cb)] = probs[:, at_cells : at_cells + cb]

    wide = lax.broadcasted_iota(jnp.int32, (rows, LANES), 1)
    rs[q] = jnp.where(wide == 0, rowv[1], rowv[2]).T[0:8]
    for p in mates:
        send(rs.at[q], rs.at[q], r_s, r_r.at[q], mate(p))

    rid = lax.broadcasted_iota(jnp.int32, (rows, 1), 0)
    first = rid < slide_rows
    position = place * slide_rows + jnp.where(first, rid, rid - slide_rows)
    count = jnp.where(first, count_ref[0], count_ref[1])
    valid = (position < count).astype(F32)
    scale_count = count.astype(F32)
    square = (slide_rows, slide_rows)
    eye = lax.broadcasted_iota(jnp.int32, square, 0) == lax.broadcasted_iota(jnp.int32, square, 1)
    counted = jnp.concatenate(
        [
            jnp.sum(jnp.where(eye, cells_ref[m : m + 1, :].astype(F32), 0.0), axis=1, keepdims=True)
            for m in range(slides)
        ],
        axis=0,
    )
    mass = rowv[0, :, 0:1]
    kcell = valid * counted

    def by_slide(value):
        return [jnp.sum(value[m * slide_rows : (m + 1) * slide_rows], axis=0, keepdims=True) for m in range(slides)]

    mass_parts = by_slide(valid * mass)
    cell_parts = by_slide(kcell)
    lane = lax.broadcasted_iota(jnp.int32, (1, LANES), 1)
    scalars = jnp.zeros((1, LANES), F32)
    for at, value in enumerate(mass_parts + cell_parts):
        scalars = jnp.where(lane == at, value, scalars)
    for m in range(slides):
        pltpu.make_async_copy(spatial_ref.at[m], tg.at[half(m)], loc.at[slides + m]).wait()

    head = backward_widths[0]
    t0[q] = tg[:, 0:head]
    for p in mates:
        send(t0.at[q], t0.at[q], t0_s, t0_r.at[q], mate(p))
    sacc[...] = jnp.zeros_like(sacc)
    s1[q, 3 * slides :, :] = jnp.zeros((8 - 3 * slides, genes), F32)
    s1[q, 3 * slides : 3 * slides + 1, 0:LANES] = scalars

    def share_logits():
        for p in (mates[1], mates[2], mates[0]):
            here = ab.at[p, half(core)]
            arrived(here, a_r.at[p])
            send(here, here, a2_s, a2_r.at[p], sibling)

    def lay_probs(p, at, value):
        af[p, at, :] = value
        there = pl.ds(pl.multiple_of(p * rows + at.start, BLOCK), BLOCK)
        probs_3[there, :] = threefold(value)

    def take_probs():
        in_blocks(0, rows, lambda at: lay_probs(q, at, pq[q, at, :]))
        for p in (mates[1], mates[2], mates[0]):
            arrived(rs.at[p], r_r.at[p])
            arrived(ab.at[p, half(1 - core)], a2_r.at[p])
            rowv[1] = jnp.concatenate([rs[p].T, jnp.zeros((rows, LANES - 8), F32)], axis=1)

            def take(at):
                probs = jnp.exp(ab[p, at, :] - rowv[1, at, 0:1]) * rowv[1, at, 1:2]
                lay_probs(p, at, probs)

            in_blocks(0, rows, take)

    def transpose(part):
        @pl.loop(0, PLANE // 2)
        def _(step):
            p = part * (PLANE // 2) + step
            high, low_part = halves(af[p].T)
            for third, value in enumerate((high, high, low_part)):
                turned_3[:, pl.ds(pl.multiple_of(third * PLANE * rows + p * rows, rows), rows)] = value

    def in_blocks(start, count, body):
        @pl.loop(0, count // BLOCK)
        def _(step):
            body(pl.ds(pl.multiple_of(start + step * BLOCK, BLOCK), BLOCK))

    quarter = lines * cb

    def lay_factor(at, length, width, value):
        high, low_part = halves(value)
        for third, part in enumerate((high, low_part, high)):
            here = pl.ds(pl.multiple_of(third * length + at.start, BLOCK), BLOCK)
            factor[here, 0:width] = part

    def keep_expr(k, at, value):
        start = sum(forward_widths[:k])
        for turn in range(turns):
            origin, width = sum(backward_widths[:turn]), backward_widths[turn]
            lo, hi = max(start, origin), min(start + forward_widths[k], origin + width)
            if lo < hi:
                high, low_part = halves(value[:, lo - start : hi - start])
                for third, part in enumerate((high, low_part, high)):
                    expr_3[at, pl.ds(3 * origin + third * width + lo - origin, hi - lo)] = part

    def three_turn_cols(k):
        return pl.ds(3 * sum(backward_widths[:k]), 3 * backward_widths[k])

    def forward_product(k):
        width = forward_widths[k]

        def lay(at):
            value = bb[k][at, :]
            lay_factor(at, quarter, width, value)
            keep_expr(k, at, value)

        in_blocks(0, quarter, lay)
        if k < chunks - 1:

            @pl.loop(0, PLANE * rows // TALL)
            def _(step):
                tall = pl.ds(pl.multiple_of(step * TALL, TALL), TALL)
                cs[k][tall, :] = product(probs_3[tall, :], factor[0 : 3 * quarter, 0:width], ((1,), (0,)))

            for p in mates:
                pass_pred(k, p)
        else:
            for side, served in ((1 - row, (mates[0], mates[2])), (row, (mates[1],))):
                pair = pl.ds(pl.multiple_of(2 * side * rows, 2 * rows), 2 * rows)
                cs[k][pair, :] = product(probs_3[pair, :], factor[0 : 3 * quarter, 0:width], ((1,), (0,)))
                for p in served:
                    pass_pred(k, p)

    def pass_pred(k, p):
        send(cs[k].at[share(p)], cr[k].at[q], c_s.at[k], c_r.at[k, q], mate(p))

    def finish_pred(k):
        total = cs[k][share(q), :]
        for p in mates:
            arrived(cr[k].at[p], c_r.at[k, p])
            total = total + cr[k][p]
        pr[:, cols(k)] = total
        if k == 0:
            p0[q] = total[:, 0:head]
            for p in mates:
                send(p0.at[q], p0.at[q], p0_s, p0_r.at[q], mate(p))
        truth = tg[:, cols(k)]
        for at, value in enumerate((total * truth, total * total, truth * truth)):
            sacc[at] += lane_groups(value)
        kept = valid * total
        stats = by_slide(kept * truth) + by_slide(kept * total) + by_slide(valid * truth * truth)
        s1[q, 0 : 3 * slides, cols(k)] = jnp.concatenate(stats, axis=0)

    early = sum(forward_widths[:EARLY])
    parts = (pl.ds(0, early), pl.ds(early, genes - early))

    def sum_plane(at):
        for p in mates:
            send(s1.at[q, :, parts[at]], s1.at[q, :, parts[at]], s1_s, s1_r.at[at, q], mate(p))

    def sum_line(at):
        for p in mates:
            arrived(s1.at[p, :, parts[at]], s1_r.at[at, p])
        s2[z, :, parts[at]] = (s1[0, :, parts[at]] + s1[1, :, parts[at]]) + (s1[2, :, parts[at]] + s1[3, :, parts[at]])
        for o in others:
            send(s2.at[z, :, parts[at]], s2.at[z, :, parts[at]], s2_s, s2_r.at[at, z], (o * PLANE + q, core))

    kept = {}

    def finish_genes(at):
        for o in others:
            arrived(s2.at[o, :, parts[at]], s2_r.at[at, o])
        total = s2[0, :, parts[at]]
        for line in range(1, lines):
            total = total + s2[line, :, parts[at]]
        gene_dot, gene_pred, gene_true = total[0:2], total[2:4], total[4:6]
        gene_inv = lax.rsqrt(gene_pred * gene_true + tiny)
        cos_gene = gene_dot * gene_inv
        gv[0:2, parts[at]] = gene_inv
        gv[2:4, parts[at]] = cos_gene * gene_true / (gene_pred * gene_true + tiny)
        kept["genes", at] = jnp.sum(jnp.sum(cos_gene, axis=1, keepdims=True), axis=0, keepdims=True)
        if at == 0:
            kept["mass"] = jnp.where(first, total[6:7, 0:1], total[6:7, 1:2])
            kept["cells"] = jnp.where(first, total[6:7, 2:3], total[6:7, 3:4])

    def sum_cores():
        sums = [jnp.sum(sacc[at], axis=1, keepdims=True) for at in range(3)]
        ss[core] = jnp.where(wide == 0, sums[0], jnp.where(wide == 1, sums[1], sums[2])).T[0:8]
        send(ss.at[core], ss.at[core], ss_s, ss_r, sibling)

    def finish_spots():
        lane_id = lax.broadcasted_iota(jnp.int32, (1, rows), 1)
        first_lane = lane_id < slide_rows
        lane_position = place * slide_rows + jnp.where(first_lane, lane_id, lane_id - slide_rows)
        lane_valid = (lane_position < jnp.where(first_lane, count_ref[0], count_ref[1])).astype(F32)
        arrived(ss.at[1 - core], ss_r)
        spot = ss[0] + ss[1]
        spot_dot, spot_pred, spot_true = spot[0:1], spot[1:2], spot[2:3]
        spot_inv = lax.rsqrt(spot_pred * spot_true + tiny)
        cos_spot = spot_dot * spot_inv
        spot_back = cos_spot * spot_true / (spot_pred * spot_true + tiny)
        kept["cos"] = jnp.sum(lane_valid * cos_spot, axis=1, keepdims=True)
        vectors = [lane_valid * spot_inv, lane_valid * spot_back, lane_valid, jnp.zeros((5, rows), F32)]
        vr[q] = jnp.concatenate(vectors, axis=0)
        sacc[0] = jnp.zeros_like(sacc[0])

    def gradient(truth, guess, by_row, k):
        pieces = []
        for m in range(slides):
            lo, hi = m * slide_rows, (m + 1) * slide_rows
            inverse, back = gv[m : m + 1, turn_cols(k)], gv[2 + m : 3 + m, turn_cols(k)]
            spot_inv, spot_back, spot_valid = by_row[lo:hi, 0:1], by_row[lo:hi, 1:2], by_row[lo:hi, 2:3]
            pieces.append(
                guess[lo:hi] * (spot_valid * back + spot_back) - truth[lo:hi] * (spot_valid * inverse + spot_inv)
            )
        return jnp.concatenate(pieces, axis=0)

    def head_gradient():
        for p in mates:
            arrived(t0.at[p], t0_r.at[p])
            arrived(p0.at[p], p0_r.at[p])
            arrived(vr.at[p], vr_r.at[p])
        for p in range(PLANE):
            ds[0][share(p), :] = gradient(t0[p], p0[p], vr[p].T, 0)
        sacc[0] += lane_groups(ds[0][share(q), :] * p0[q])

    def send_grad(k):
        if k == 0:
            for p in mates:
                send(vr.at[q], vr.at[q], vr_s, vr_r.at[q], mate(p))
            kept["by_row"] = vr[q].T
            return
        grad = gradient(tg[:, turn_cols(k)], pr[:, turn_cols(k)], kept["by_row"], k)
        here = ds[k].at[share(q)]
        here[...] = grad
        for p in mates:
            send(here, here, d_s.at[k], d_r.at[k, q], mate(p))
        sacc[0] += lane_groups(grad * pr[:, turn_cols(k)])

    def send_terms():
        mass_total, cell_total = kept["mass"], kept["cells"]
        portion = kcell / cell_total
        kl_rows = portion * (jnp.log(counted) - jnp.log(cell_total) - jnp.log(mass) + jnp.log(mass_total))
        dmass = scale_count * valid * (1.0 / mass_total - portion / mass)
        terms = jnp.sum(scale_count * kl_rows, axis=0, keepdims=True) - kept["cos"]
        l1[q] = jnp.broadcast_to(terms, (8, LANES))
        for p in mates:
            send(l1.at[q], l1.at[q], l1_s, l1_r.at[q], mate(p))
        inner = jnp.sum(sacc[0], axis=1, keepdims=True)
        inn[core] = jnp.where(wide == 0, inner, kept["genes", 0] + kept["genes", 1])
        send(inn.at[core], inn.at[core], in_s, in_r, sibling)
        rowv[1] = jnp.broadcast_to(dmass, (rows, LANES))

    middle = lines // 2

    def backward_product(k):
        if k == 0:
            head_gradient()
        else:
            for p in mates:
                arrived(ds[k].at[share(p)], d_r.at[k, p])
        width, spots = backward_widths[k], PLANE * rows

        def lay(at):
            value = ds[k][at, :]
            lay_factor(at, spots, width, value)
            grad_3[at, three_turn_cols(k)] = threefold(value)

        in_blocks(0, spots, lay)
        if not halved(k):

            @pl.loop(0, quarter // TALL)
            def _(step):
                tall = pl.ds(pl.multiple_of(step * TALL, TALL), TALL)
                es[k][tall, :] = product(turned_3[tall, :], factor[0 : 3 * spots, 0:width], ((1,), (0,)))

        for turn in range(2):
            if halved(k):
                side = (1 - z // middle) if turn == 0 else z // middle
                pair = pl.ds(pl.multiple_of(side * middle * cb, middle * cb), middle * cb)
                es[k][pair, :] = product(turned_3[pair, :], factor[0 : 3 * spots, 0:width], ((1,), (0,)))

            @pl.when(z == 0)
            def _():
                if halved(k):
                    pass_up(k, middle if turn == 0 else 1, middle if turn == 0 else middle - 1, turn)
                elif whole(k):
                    if turn == 0:
                        pass_up(k, 1, last, 0)
                elif turn == 0:
                    for line in range(last, 0, -1):
                        pass_up(k, line, 1, line)

            @pl.when(z == last)
            def _():
                if halved(k):
                    pass_down(k, 0 if turn == 0 else middle, middle if turn == 0 else middle - 1, turn)
                elif whole(k):
                    if turn == 0:
                        pass_down(k, 0, last, 0)
                elif turn == 0:
                    for line in range(last):
                        pass_down(k, line, 1, line)

    def halved(k):
        return k == 0

    def whole(k):
        return 0 < k < turns - SPLIT

    def pass_up(k, line, count, slot):
        here = pl.ds(line * cb, count * cb)
        send(es[k].at[here], ru[k].at[here], ru_s.at[k], ru_r.at[k, slot], up)

    def pass_down(k, line, count, slot):
        here = pl.ds(line * cb, count * cb)
        send(es[k].at[here], rd[k].at[here], rd_s.at[k], rd_r.at[k, slot], down)

    def take_up(k, line, count, slot):
        arrived(ru[k].at[pl.ds(line * cb, count * cb)], ru_r.at[k, slot])

    def take_down(k, line, count, slot):
        arrived(rd[k].at[pl.ds(line * cb, count * cb)], rd_r.at[k, slot])

    def add_up(k, line, count):
        def add(at):
            es[k][at, :] += ru[k][at, :]

        in_blocks(line * cb, count * cb, add)

    def add_down(k, line, count):
        def add(at):
            es[k][at, :] += rd[k][at, :]

        in_blocks(line * cb, count * cb, add)

    def rising(k, at):
        if halved(k) or whole(k):
            start = middle if halved(k) else at
            take_up(k, start, lines - start, 0)
            above = max(at + 1, start)
            add_up(k, above, lines - above)
            pass_up(k, above, lines - above, 0)
        else:
            for line in range(last, at, -1):
                take_up(k, line, 1, line)
                add_up(k, line, 1)
                pass_up(k, line, 1, line)

    def falling(k, at):
        if halved(k) or whole(k):
            end = middle if halved(k) else at + 1
            take_down(k, 0, end, 0)
            below = min(at, end)
            add_down(k, 0, below)
            pass_down(k, 0, below, 0)
        else:
            for line in range(at):
                take_down(k, line, 1, line)
                add_down(k, line, 1)
                pass_down(k, line, 1, line)

    def add_near(k):
        for at in range(1, last):

            @pl.when(z == at)
            def _():
                (rising if low(at) else falling)(k, at)

    def add_far(k):
        for at in range(1, last):

            @pl.when(z == at)
            def _():
                (falling if low(at) else rising)(k, at)

    def finish_expr(k):
        for at in range(lines):

            @pl.when(z == at)
            def _():
                if at > 0:
                    if halved(k) and at < middle:
                        take_up(k, at, 1, 1)
                    elif at == last and (halved(k) or whole(k)):
                        take_up(k, at, 1, 0)
                    elif not halved(k) and not whole(k):
                        take_up(k, at, 1, at)
                if at < last:
                    if halved(k) and at >= middle:
                        take_down(k, at, 1, 1)
                    elif at == 0 and (halved(k) or whole(k)):
                        take_down(k, at, 1, 0)
                    elif not halved(k) and not whole(k):
                        take_down(k, at, 1, at)

        from_low, from_high = z > 0, z < last

        @pl.loop(0, cb // BLOCK)
        def _(step):
            here = pl.ds(pl.multiple_of(step * BLOCK, BLOCK), BLOCK)
            own = pl.ds(pl.multiple_of(z * cb + step * BLOCK, BLOCK), BLOCK)
            total = es[k][own, :]
            total = total + jnp.where(from_low, ru[k][own, :], 0.0)
            ge[here, turn_cols(k)] = total + jnp.where(from_high, rd[k][own, :], 0.0)

    def probs_gradient(k):
        at = three_turn_cols(k)

        @pl.loop(0, PLANE * rows // TALL)
        def _(step):
            tall = pl.ds(pl.multiple_of(step * TALL, TALL), TALL)
            part = product(grad_3[tall, at], expr_3[:, at], ((1,), (1,)))
            if k == 0:
                fs[tall, :] = part
            else:
                fs[tall, :] += part

    def slide_of(p, m):
        return pl.ds(pl.multiple_of(p * rows + m * slide_rows, slide_rows), slide_rows)

    def sum_probs_cores():
        for p in mates + (q,):
            fx[p] = fs[slide_of(p, 1 - core), :]
            send(fx.at[p], fy.at[p], fx_s, fx_r.at[p], sibling)

    def return_probs():
        for p in mates:
            arrived(fy.at[p], fx_r.at[p])
            fz[p] = fs[slide_of(p, core), :] + fy[p]
            send(fz.at[p], fr.at[q], f_s, f_r.at[q], mate(p))
        arrived(fy.at[q], fx_r.at[q])
        fr[q] = fs[slide_of(q, core), :] + fy[q]

    def pass_terms():
        for p in mates:
            arrived(l1.at[p], l1_r.at[p])
        l2[z] = (l1[0] + l1[1]) + (l1[2] + l1[3])
        for o in others:
            send(l2.at[z], l2.at[z], l2_s, l2_r.at[z], (o * PLANE + q, core))

    def part_of(slide, m):
        start = slide * slide_rows + m * (slide_rows // 2)
        return pl.ds(pl.multiple_of(start, slide_rows // 2), slide_rows // 2)

    def finish_logits():
        arrived(inn.at[1 - core], in_r)
        rowv[2] = (inn[0] + inn[1]) + rowv[1] * rowv[0]
        for p in mates:
            arrived(fr.at[p], f_r.at[p])
        for m in range(2):

            @pl.loop(0, slide_rows // STEP_ROWS // 2)
            def _(step):
                row_at = (m * (slide_rows // STEP_ROWS // 2) + step) * STEP_ROWS
                at = pl.ds(pl.multiple_of(row_at, STEP_ROWS), STEP_ROWS)
                whole_at = pl.ds(pl.multiple_of(core * slide_rows + row_at, STEP_ROWS), STEP_ROWS)
                by_mass, total_inner = rowv[1, whole_at, 0:1], rowv[2, whole_at, 0:1]
                for p in range(PLANE):
                    for line in range(lines):
                        here, there = pl.ds(line * cb, cb), (line * PLANE + p) * cb
                        grad = fr[p, at, here] + by_mass * weights[:, there : there + cb]
                        glog[whole_at, pl.ds(there, cb)] = pq[p, whole_at, here] * (grad - total_inner)

            here = part_of(core, m)
            send(glog.at[here], glog.at[here], go_s, go_r.at[m], sibling)

    def forward_left():
        for k in range(chunks):

            @pl.when(z < last)
            def _():
                sent(bb[k].at[block(z)], ou_s.at[k])

            @pl.when(z > 0)
            def _():
                sent(bb[k].at[block(z)], od_s.at[k])

            for at in range(1, last):

                @pl.when(z == at)
                def _():
                    sent(bb[k].at[pl.ds(0, at * cb)], fu_s.at[k])
                    sent(bb[k].at[pl.ds((at + 1) * cb, (last - at) * cb)], fd_s.at[k])

        three = pl.ds(0, len(mates))
        sent(ab.at[three, half(0)], a_s)
        sent(ab.at[three, half(0)], a2_s)
        sent(rs.at[three], r_s)
        sent(t0.at[three], t0_s)
        sent(p0.at[three], p0_s)
        for k in range(chunks):
            sent(cr[k].at[three], c_s.at[k])
        sent(s1.at[three], s1_s)
        sent(s2.at[pl.ds(0, last)], s2_s)
        sent(ss.at[0], ss_s)

    steps = {
        "far": forward_far,
        "near": forward_near,
        "share": share_logits,
        "take": take_probs,
        "whole": gathered,
        "product": forward_product,
        "sum": finish_pred,
        "turn": transpose,
        "plane": sum_plane,
        "line": sum_line,
        "genes": finish_genes,
        "cores": sum_cores,
        "spots": finish_spots,
        "grad": send_grad,
        "terms": send_terms,
        "backward": backward_product,
        "probs": probs_gradient,
        "exchange": sum_probs_cores,
        "return": return_probs,
        "loss": pass_terms,
        "logits": finish_logits,
        "add_near": add_near,
        "add_far": add_far,
        "expr": finish_expr,
        "left": forward_left,
    }
    for name, *where in STEPS:
        steps[name](*where)

    for o in others:
        arrived(l2.at[o], l2_r.at[o])
    loss = l2[0]
    for line in range(1, lines):
        loss = loss + l2[line]
    loss_ref[...] = loss[0:1, 0:1] - (inn[0, 0:1, 1:2] + inn[1, 0:1, 1:2])
    for m in range(2):
        arrived(glog.at[part_of(1 - core, m)], go_r.at[m])

    for k in range(turns):
        for at in range(lines):

            @pl.when(z == at)
            def _():
                if at < last:
                    sent(es[k].at[pl.ds((at + 1) * cb, (last - at) * cb)], ru_s.at[k])
                if at > 0:
                    sent(es[k].at[pl.ds(0, at * cb)], rd_s.at[k])

    three = pl.ds(0, len(mates))
    for k in range(1, turns):
        sent(ds[k].at[pl.ds(0, len(mates) * rows)], d_s.at[k])
    sent(vr.at[three], vr_s)
    sent(inn.at[0], in_s)
    sent(l1.at[three], l1_s)
    sent(l2.at[pl.ds(0, last)], l2_s)
    sent(fr.at[three], f_s)
    sent(fx, fx_s)
    sent(glog.at[half(0)], go_s)


def lane_groups(value):
    parts = [value[:, at : at + LANES] for at in range(0, value.shape[1], LANES)]
    return functools.reduce(lambda a, b: a + b, parts)


def grouped(refs, sizes):
    at = 0
    for size in sizes:
        yield refs[at : at + size]
        at += size


def deliver(pred_in, loss_in, glog_in, gexp_in, pred_ref, loss_ref, glog_ref, gexp_ref, sems):
    slides, slide_rows = pred_ref.shape[0], pred_ref.shape[1]
    pairs = [(gexp_in, gexp_ref), (loss_in, loss_ref)]
    for m in range(slides):
        part = pl.ds(m * slide_rows, slide_rows)
        pairs += [(glog_in.at[part], glog_ref.at[m]), (pred_in.at[part], pred_ref.at[m])]
    copies = [pltpu.make_async_copy(src, dst, sems.at[at]) for at, (src, dst) in enumerate(pairs)]
    for copy in copies:
        copy.start()
    for copy in copies:
        copy.wait()


def plane_call(logits, expr, spatial, slide_spots, spot_cells, cell_prior, lines):
    slides, slide_rows, cells = logits.shape
    rows = slides * slide_rows
    cb, genes = expr.shape
    quarter = lines * cb
    spots = PLANE * rows
    chunks, turns = len(FORWARD), len(BACKWARD)
    dma = pltpu.SemaphoreType.DMA
    vmem = pltpu.VMEM
    anywhere = pl.BlockSpec(memory_space=pl.ANY)
    in_vmem = pl.BlockSpec(memory_space=pltpu.VMEM)
    scratch = [
        pltpu.SMEM((slides,), jnp.int32),
        vmem((slides, slide_rows), jnp.int32),
        vmem((1, cells), jnp.int32),
        vmem((rows, cells), F32),
        vmem((PLANE, slide_rows, quarter), F32),
        vmem((rows, genes), F32),
        vmem((cb, genes), F32),
        vmem((PLANE, rows, quarter), F32),
        vmem((PLANE, rows, quarter), F32),
        vmem((PLANE, rows, quarter), F32),
        vmem((spots, 3 * quarter), BF16),
        vmem((quarter, 3 * spots), BF16),
        vmem((quarter, 3 * genes), BF16),
        vmem((3, rows, LANES), F32),
        vmem((PLANE, 8, genes), F32),
        vmem((lines, 8, genes), F32),
        vmem((8, genes), F32),
        vmem((2, 8, rows), F32),
        vmem((3, rows, LANES), F32),
        vmem((PLANE, 8, rows), F32),
        vmem((spots, 3 * genes), BF16),
        vmem((3 * max(quarter, spots), max(FORWARD + BACKWARD)), BF16),
        vmem((PLANE, rows, BACKWARD[0]), F32),
        vmem((PLANE, rows, BACKWARD[0]), F32),
        vmem((PLANE, 8, rows), F32),
        vmem((spots, quarter), F32),
        vmem((PLANE, slide_rows, quarter), F32),
        vmem((PLANE, slide_rows, quarter), F32),
        vmem((PLANE, slide_rows, quarter), F32),
        vmem((PLANE, slide_rows, quarter), F32),
        vmem((2, rows, LANES), F32),
        vmem((PLANE, 8, LANES), F32),
        vmem((lines, 8, LANES), F32),
        dma((2 * slides + 4,)),
        dma((chunks,)),
        dma((chunks,)),
        dma((chunks,)),
        dma((chunks,)),
        dma((chunks,)),
        dma((chunks,)),
        dma((chunks,)),
        dma((chunks,)),
        dma,
        dma((PLANE,)),
        dma,
        dma((PLANE,)),
        dma,
        dma((PLANE,)),
        dma((chunks,)),
        dma((chunks, PLANE)),
        dma,
        dma((2, PLANE)),
        dma,
        dma((2, lines)),
        dma,
        dma,
        dma((turns,)),
        dma((turns, PLANE)),
        dma((turns,)),
        dma((turns, lines)),
        dma((turns,)),
        dma((turns, lines)),
        dma,
        dma((PLANE,)),
        dma,
        dma((PLANE,)),
        dma,
        dma((2,)),
        dma,
        dma,
        dma,
        dma((PLANE,)),
        dma,
        dma((lines,)),
        dma,
        dma((PLANE,)),
        dma,
        dma((PLANE,)),
        dma,
        dma((PLANE,)),
    ]
    for shape, widths in (
        ((quarter,), FORWARD),
        ((spots,), FORWARD),
        ((PLANE, rows), FORWARD),
        ((spots,), BACKWARD),
        ((quarter,), BACKWARD),
        ((quarter,), BACKWARD),
        ((quarter,), BACKWARD),
    ):
        scratch += [vmem(shape + (width,), F32) for width in widths]
    in_hbm = functools.partial(pltpu.with_memory_space_constraint, memory_space=pltpu.HBM)
    in_place = functools.partial(pltpu.with_memory_space_constraint, memory_space=pltpu.VMEM)
    results = pl.pallas_call(
        functools.partial(plane_kernel, lines, FORWARD, BACKWARD),
        out_shape=(
            vmem((rows, genes), F32),
            vmem((1, 1), F32),
            vmem((rows, cells), F32),
            vmem((cb, genes), F32),
        ),
        in_specs=[anywhere] * 6,
        out_specs=(in_vmem,) * 4,
        scratch_shapes=scratch,
        compiler_params=pltpu.CompilerParams(
            collective_id=0, has_side_effects=True, vmem_limit_bytes=48 * 1024 * 1024
        ),
    )(*map(in_hbm, (logits, expr, spatial, slide_spots, spot_cells, cell_prior.reshape(1, cells))))
    pred, loss, grad_logits, grad_expr = pl.pallas_call(
        deliver,
        out_shape=(
            jax.ShapeDtypeStruct((slides, slide_rows, genes), F32),
            jax.ShapeDtypeStruct((1, 1), F32),
            jax.ShapeDtypeStruct((slides, slide_rows, cells), F32),
            jax.ShapeDtypeStruct((cb, genes), F32),
        ),
        in_specs=[anywhere] * 4,
        out_specs=(anywhere,) * 4,
        scratch_shapes=[dma((2 * slides + 2,))],
        compiler_params=pltpu.CompilerParams(vmem_limit_bytes=4 * 1024 * 1024),
    )(*map(in_place, results))
    return pred, loss.reshape(()), grad_logits, grad_expr


def general_plan(logits, expr, spatial, slide_spots, spot_cells, cell_prior):
    place = lax.axis_index("spot")
    side = lax.axis_index("gene")
    rows_all = logits.shape[1]
    cell_rows = expr.shape[0]
    weights = cell_prior.astype(jnp.float32) / fixed_point
    gene_share = (place == 0).astype(jnp.float32)
    row_share = (side == 0).astype(jnp.float32)
    own_weights = lax.dynamic_slice_in_dim(weights, place * cell_rows, cell_rows, 0)
    expr_acc = jnp.zeros((cell_rows, expr.shape[1]), jnp.float32)
    loss_local = jnp.zeros((), jnp.float32)
    pred_list = []
    grad_list = []
    for slide in range(logits.shape[0]):
        logit_rows = logits[slide]
        counted = spot_cells[slide].astype(jnp.float32)
        target = spatial[slide]
        positions = place * rows_all + jnp.arange(rows_all, dtype=jnp.int32)
        valid = (positions < slide_spots[slide]).astype(jnp.float32)
        peak = jnp.max(logit_rows, axis=1, keepdims=True)
        raised = jnp.exp(logit_rows - peak)
        probs = raised / jnp.sum(raised, axis=1, keepdims=True)
        mass = jnp.dot(probs, weights, precision=lax.Precision.HIGHEST)
        blocks = lax.all_to_all(probs, "spot", split_axis=1, concat_axis=0, tiled=True)
        pred = lax.psum_scatter(
            jnp.dot(blocks, expr, precision=lax.Precision.HIGHEST),
            "spot",
            scatter_dimension=0,
            tiled=True,
        )
        gene_dot = jnp.sum(valid[:, None] * pred * target, axis=0)
        gene_pred = jnp.sum(valid[:, None] * pred * pred, axis=0)
        gene_true = jnp.sum(valid[:, None] * target * target, axis=0)
        mass_part = jnp.sum(valid * mass)
        kcell = valid * counted
        cell_part = jnp.sum(kcell)
        spot_dot = jnp.sum(pred * target, axis=1)
        spot_pred = jnp.sum(pred * pred, axis=1)
        spot_true = jnp.sum(target * target, axis=1)
        gene_dot, gene_pred, gene_true, mass_total, cell_total = lax.psum(
            (gene_dot, gene_pred, gene_true, mass_part, cell_part), "spot"
        )
        spot_dot, spot_pred, spot_true = lax.psum((spot_dot, spot_pred, spot_true), "gene")
        gene_inv = lax.rsqrt(gene_pred * gene_true + tiny)
        cos_gene = gene_dot * gene_inv
        spot_inv = lax.rsqrt(spot_pred * spot_true + tiny)
        cos_spot = spot_dot * spot_inv
        share = kcell / cell_total
        scale_count = slide_spots[slide].astype(jnp.float32)
        kl_part = jnp.sum(
            share * (jnp.log(counted) - jnp.log(cell_total) - jnp.log(mass) + jnp.log(mass_total))
        )
        loss_local = loss_local - gene_share * jnp.sum(cos_gene)
        loss_local = loss_local + row_share * (scale_count * kl_part - jnp.sum(valid * cos_spot))
        gene_back = cos_gene * gene_true / (gene_pred * gene_true + tiny)
        spot_back = cos_spot * spot_true / (spot_pred * spot_true + tiny)
        dpred = -valid[:, None] * (
            target * (gene_inv[None, :] + spot_inv[:, None])
            - pred * gene_back[None, :]
            - pred * spot_back[:, None]
        )
        dmass = scale_count * valid * (1.0 / mass_total - share / mass)
        pred_list.append(pred)
        grads_full, mass_full = (
            lax.all_gather(dpred, "spot", axis=0, tiled=True),
            lax.all_gather(dmass, "spot", axis=0, tiled=True),
        )
        dprob_cells = jnp.dot(grads_full, expr.T, precision=lax.Precision.HIGHEST)
        dprob_cells = lax.psum(dprob_cells, "gene")
        expr_acc = expr_acc + lax.dot_general(
            blocks, grads_full, (((0,), (0,)), ((), ())), precision=lax.Precision.HIGHEST
        )
        dprob_cells = dprob_cells + mass_full[:, None] * own_weights[None, :]
        dprob_rows = lax.all_to_all(dprob_cells, "spot", split_axis=0, concat_axis=1, tiled=True)
        inner = jnp.sum(probs * dprob_rows, axis=1, keepdims=True)
        dlogit = probs * (dprob_rows - inner)
        grad_list.append(dlogit)
    loss = lax.psum(loss_local, ("spot", "gene"))
    return (jnp.stack(pred_list), loss, jnp.stack(grad_list), expr_acc)


def solution(mesh):
    places = mesh.shape["spot"]

    def on_device(logits, expr, spatial, slide_spots, spot_cells, cell_prior):
        if places == PLANE * PLANE and mesh.shape["gene"] == 2 and expr.shape[1] == sum(FORWARD):
            return plane_call(
                logits, expr, spatial, slide_spots, spot_cells, cell_prior, places // PLANE
            )
        return general_plan(logits, expr, spatial, slide_spots, spot_cells, cell_prior)

    in_specs = (
        P(None, "spot", None),
        P("spot", "gene"),
        P(None, "spot", "gene"),
        P(),
        P(None, "spot"),
        P(),
    )
    out_specs = (P(None, "spot", "gene"), P(), P(None, "spot", None), P("spot", "gene"))
    return jax.shard_map(
        on_device, mesh=mesh, in_specs=in_specs, out_specs=out_specs, check_vma=False
    )
```

```python
import functools

import jax
import jax.numpy as jnp
from jax import lax
from jax.experimental import pallas as pl
from jax.experimental.pallas import tpu as pltpu
from jax.sharding import PartitionSpec as P

tiny = 1e-06
fixed_point = 16384.0
F32 = jnp.float32
BF16 = jnp.bfloat16
MESH = pl.DeviceIdType.MESH

PLANE = 4
LANES = 128
STEP_ROWS = 16
BLOCK = 32
TALL = 256
FORWARD = (128, 256, 256, 128, 128, 128)
BACKWARD = (128, 128, 256, 256, 256)
SPLIT = 4
LEAD = 1
NEAR_LEAD = 3
EARLY = 3
STEPS = (
    ("far", 0),
    ("far", 1),
    ("near", 0),
    ("share",),
    ("far", 2),
    ("far", 3),
    ("take",),
    ("whole", 0),
    ("near", 1),
    ("product", 0),
    ("sum", 0),
    ("whole", 1),
    ("near", 2),
    ("product", 1),
    ("whole", 2),
    ("product", 2),
    ("whole", 3),
    ("near", 3),
    ("product", 3),
    ("far", 4),
    ("whole", 4),
    ("near", 4),
    ("product", 4),
    ("sum", 1),
    ("turn", 0),
    ("far", 5),
    ("whole", 5),
    ("near", 5),
    ("product", 5),
    ("sum", 2),
    ("plane", 0),
    ("turn", 1),
    ("sum", 3),
    ("line", 0),
    ("sum", 4),
    ("sum", 5),
    ("plane", 1),
    ("cores",),
    ("genes", 0),
    ("spots",),
    ("grad", 0),
    ("grad", 1),
    ("grad", 2),
    ("line", 1),
    ("backward", 0),
    ("backward", 1),
    ("add_near", 0),
    ("genes", 1),
    ("grad", 3),
    ("backward", 2),
    ("probs", 0),
    ("add_far", 0),
    ("probs", 1),
    ("expr", 0),
    ("grad", 4),
    ("add_near", 1),
    ("probs", 2),
    ("terms",),
    ("backward", 3),
    ("probs", 3),
    ("add_near", 2),
    ("backward", 4),
    ("add_far", 1),
    ("probs", 4),
    ("exchange",),
    ("add_near", 3),
    ("add_far", 2),
    ("left",),
    ("return",),
    ("loss",),
    ("add_far", 3),
    ("expr", 1),
    ("add_near", 4),
    ("logits",),
    ("add_far", 4),
    ("expr", 2),
    ("expr", 3),
    ("expr", 4),
)


def halves(value):
    high = value.astype(BF16)
    return high, (value - high.astype(F32)).astype(BF16)


def threefold(value):
    high, low = halves(value)
    return jnp.concatenate([high, high, low], axis=1)


def product(a, b, contract):
    return lax.dot_general(a, b, (contract, ((), ())), preferred_element_type=F32)


def plane_kernel(lines, forward_widths, backward_widths, *refs):
    chunks, turns = len(forward_widths), len(backward_widths)
    (
        (logits_ref, expr_ref, spatial_ref, count_in, cells_in, prior_in),
        (pr, loss_ref, glog, ge),
        (count_ref, cells_ref, prior_ref, lg, lq, tg, ex, pq, ab, af, probs_3, turned_3, expr_3, sacc, s1, s2, gv, ss, rowv, rs),
        (grad_3, factor, t0, p0, vr, fs, fx, fy, fz, fr, inn, l1, l2),
        (loc, ou_s, ou_r, od_s, od_r, fu_s, fu_r, fd_s, fd_r, a_s, a_r, a2_s, a2_r, r_s, r_r),
        (c_s, c_r, s1_s, s1_r, s2_s, s2_r, ss_s, ss_r, d_s, d_r, ru_s, ru_r, rd_s, rd_r),
        (f_s, f_r, fx_s, fx_r, go_s, go_r, in_s, in_r, l1_s, l1_r, l2_s, l2_r, t0_s, t0_r, p0_s, p0_r, vr_s, vr_r),
        bb,
        cs,
        cr,
        ds,
        es,
        ru,
        rd,
    ) = grouped(refs, (6, 4, 20, 13, 15, 14, 18, chunks, chunks, chunks, turns, turns, turns, turns))
    place = lax.axis_index("spot")
    core = lax.axis_index("gene")
    z = place // PLANE
    q = place % PLANE
    col, row = q % 2, q // 2
    mates = ((1 - row) * 2 + 1 - col, row * 2 + 1 - col, (1 - row) * 2 + col)
    others = tuple((z + step) % lines for step in range(1, lines))
    up, down = (place + PLANE, core), (place - PLANE, core)
    sibling = (place, 1 - core)
    slides, slide_rows = logits_ref.shape[0], logits_ref.shape[1]
    rows = slides * slide_rows
    cb = expr_ref.shape[0]
    genes = expr_ref.shape[1]
    last = lines - 1

    def mate(p):
        return (z * PLANE + p, core)

    def send(src, dst, send_sem, recv_sem, device):
        copy = pltpu.make_async_remote_copy(
            src_ref=src, dst_ref=dst, send_sem=send_sem, recv_sem=recv_sem, device_id=device, device_id_type=MESH
        )
        copy.start()

    def arrived(dst, recv_sem):
        pltpu.make_async_copy(dst, dst, recv_sem).wait()

    sent = arrived

    def cols(k):
        return pl.ds(sum(forward_widths[:k]), forward_widths[k])

    def turn_cols(k):
        return pl.ds(sum(backward_widths[:k]), backward_widths[k])

    def block(index):
        return pl.ds(pl.multiple_of(index * cb, cb), cb)

    def share(index):
        return pl.ds(pl.multiple_of(index * rows, rows), rows)

    def half(index):
        return pl.ds(pl.multiple_of(index * slide_rows, slide_rows), slide_rows)

    small = ((prior_in, prior_ref), (count_in, count_ref), (cells_in, cells_ref))
    pltpu.make_async_copy(expr_ref, ex, loc.at[2 * slides]).start()
    for m in range(slides):
        pltpu.make_async_copy(logits_ref.at[m], lg.at[half(m)], loc.at[m]).start()
    for at, (src, dst) in enumerate(small):
        pltpu.make_async_copy(src, dst, loc.at[2 * slides + 1 + at]).start()
    for m in range(slides):
        pltpu.make_async_copy(spatial_ref.at[m], tg.at[half(m)], loc.at[slides + m]).start()

    barrier = pltpu.get_barrier_semaphore()
    for p in mates:
        pl.semaphore_signal(barrier, inc=1, device_id=mate(p), device_id_type=MESH)
    for o in others:
        pl.semaphore_signal(barrier, inc=1, device_id=(o * PLANE + q, core), device_id_type=MESH)
    pl.semaphore_signal(barrier, inc=1, device_id=sibling, device_id_type=MESH)
    pltpu.make_async_copy(expr_ref, ex, loc.at[2 * slides]).wait()
    for k in range(chunks):
        bb[k][block(z), :] = ex[:, cols(k)]
    for m in range(slides):
        pltpu.make_async_copy(logits_ref.at[m], lg.at[half(m)], loc.at[m]).wait()
    for p in range(PLANE):
        for line in range(lines):
            lq[p, :, pl.ds(line * cb, cb)] = lg[half(core), pl.ds((line * PLANE + p) * cb, cb)]
    pl.semaphore_wait(barrier, len(mates) + len(others) + 1)

    def own_up(k):
        here = bb[k].at[block(z)]
        send(here, here, ou_s.at[k], ou_r.at[k], up)

    def own_down(k):
        here = bb[k].at[block(z)]
        send(here, here, od_s.at[k], od_r.at[k], down)

    def low(at):
        return 2 * at < lines

    for at in range(lines):

        @pl.when(z == at)
        def _():
            for k in range(chunks):
                if at < last and (at == 0 or k < (LEAD if low(at) else NEAR_LEAD)):
                    own_up(k)
                if at > 0 and (at == last or k < (NEAR_LEAD if low(at) else LEAD)):
                    own_down(k)

    for p in mates:
        send(lq.at[p], ab.at[q, half(core)], a_s, a_r.at[q], mate(p))

    def from_below(k, at):
        arrived(bb[k].at[pl.ds((at - 1) * cb, cb)], ou_r.at[k])
        if at > 1:
            arrived(bb[k].at[pl.ds(0, (at - 1) * cb)], fu_r.at[k])

    def from_above(k, at):
        arrived(bb[k].at[pl.ds((at + 1) * cb, cb)], od_r.at[k])
        if at < last - 1:
            arrived(bb[k].at[pl.ds((at + 2) * cb, (last - 1 - at) * cb)], fd_r.at[k])

    def upward(k, at):
        from_below(k, at)
        here = bb[k].at[pl.ds(0, at * cb)]
        send(here, here, fu_s.at[k], fu_r.at[k], up)

    def downward(k, at):
        from_above(k, at)
        here = bb[k].at[pl.ds((at + 1) * cb, (last - at) * cb)]
        send(here, here, fd_s.at[k], fd_r.at[k], down)

    def forward_far(k):
        for at in range(1, last):

            @pl.when(z == at)
            def _():
                (upward if low(at) else downward)(k, at)
                if k + LEAD < chunks:
                    (own_up if low(at) else own_down)(k + LEAD)

    def forward_near(k):
        for at in range(1, last):

            @pl.when(z == at)
            def _():
                (downward if low(at) else upward)(k, at)
                if k + NEAR_LEAD < chunks:
                    (own_down if low(at) else own_up)(k + NEAR_LEAD)

    def gathered(k):
        @pl.when(z == 0)
        def _():
            from_above(k, 0)

        @pl.when(z == last)
        def _():
            from_below(k, last)

    for at, (src, dst) in enumerate(small):
        pltpu.make_async_copy(src, dst, loc.at[2 * slides + 1 + at]).wait()
    weights = prior_ref[...].astype(F32) / fixed_point

    @pl.loop(0, rows // STEP_ROWS)
    def _(step):
        at = pl.ds(pl.multiple_of(step * STEP_ROWS, STEP_ROWS), STEP_ROWS)
        value = lg[at, :]
        peak = jnp.max(value, axis=1, keepdims=True)
        raised = jnp.exp(value - peak)
        scale = 1.0 / jnp.sum(raised, axis=1, keepdims=True)
        probs = raised * scale
        mass_rows = jnp.sum(probs * weights, axis=1, keepdims=True)
        rowv[0, at, :] = jnp.broadcast_to(mass_rows, (STEP_ROWS, LANES))
        rowv[1, at, :] = jnp.broadcast_to(peak, (STEP_ROWS, LANES))
        rowv[2, at, :] = jnp.broadcast_to(scale, (STEP_ROWS, LANES))
        for p in range(PLANE):
            for line in range(lines):
                at_cells = (line * PLANE + p) * cb
                pq[p, at, pl.ds(line * cb, cb)] = probs[:, at_cells : at_cells + cb]

    wide = lax.broadcasted_iota(jnp.int32, (rows, LANES), 1)
    rs[q] = jnp.where(wide == 0, rowv[1], rowv[2]).T[0:8]
    for p in mates:
        send(rs.at[q], rs.at[q], r_s, r_r.at[q], mate(p))

    rid = lax.broadcasted_iota(jnp.int32, (rows, 1), 0)
    first = rid < slide_rows
    position = place * slide_rows + jnp.where(first, rid, rid - slide_rows)
    count = jnp.where(first, count_ref[0], count_ref[1])
    valid = (position < count).astype(F32)
    scale_count = count.astype(F32)
    square = (slide_rows, slide_rows)
    eye = lax.broadcasted_iota(jnp.int32, square, 0) == lax.broadcasted_iota(jnp.int32, square, 1)
    counted = jnp.concatenate(
        [
            jnp.sum(jnp.where(eye, cells_ref[m : m + 1, :].astype(F32), 0.0), axis=1, keepdims=True)
            for m in range(slides)
        ],
        axis=0,
    )
    mass = rowv[0, :, 0:1]
    kcell = valid * counted

    def by_slide(value):
        return [jnp.sum(value[m * slide_rows : (m + 1) * slide_rows], axis=0, keepdims=True) for m in range(slides)]

    mass_parts = by_slide(valid * mass)
    cell_parts = by_slide(kcell)
    lane = lax.broadcasted_iota(jnp.int32, (1, LANES), 1)
    scalars = jnp.zeros((1, LANES), F32)
    for at, value in enumerate(mass_parts + cell_parts):
        scalars = jnp.where(lane == at, value, scalars)
    for m in range(slides):
        pltpu.make_async_copy(spatial_ref.at[m], tg.at[half(m)], loc.at[slides + m]).wait()

    head = backward_widths[0]
    t0[q] = tg[:, 0:head]
    for p in mates:
        send(t0.at[q], t0.at[q], t0_s, t0_r.at[q], mate(p))
    sacc[...] = jnp.zeros_like(sacc)
    s1[q, 3 * slides :, :] = jnp.zeros((8 - 3 * slides, genes), F32)
    s1[q, 3 * slides : 3 * slides + 1, 0:LANES] = scalars

    def share_logits():
        for p in (mates[1], mates[2], mates[0]):
            here = ab.at[p, half(core)]
            arrived(here, a_r.at[p])
            send(here, here, a2_s, a2_r.at[p], sibling)

    def lay_probs(p, at, value):
        af[p, at, :] = value
        there = pl.ds(pl.multiple_of(p * rows + at.start, BLOCK), BLOCK)
        probs_3[there, :] = threefold(value)

    def take_probs():
        in_blocks(0, rows, lambda at: lay_probs(q, at, pq[q, at, :]))
        for p in (mates[1], mates[2], mates[0]):
            arrived(rs.at[p], r_r.at[p])
            arrived(ab.at[p, half(1 - core)], a2_r.at[p])
            rowv[1] = jnp.concatenate([rs[p].T, jnp.zeros((rows, LANES - 8), F32)], axis=1)

            def take(at):
                probs = jnp.exp(ab[p, at, :] - rowv[1, at, 0:1]) * rowv[1, at, 1:2]
                lay_probs(p, at, probs)

            in_blocks(0, rows, take)

    def transpose(part):
        @pl.loop(0, PLANE // 2)
        def _(step):
            p = part * (PLANE // 2) + step
            high, low_part = halves(af[p].T)
            for third, value in enumerate((high, high, low_part)):
                turned_3[:, pl.ds(pl.multiple_of(third * PLANE * rows + p * rows, rows), rows)] = value

    def in_blocks(start, count, body):
        @pl.loop(0, count // BLOCK)
        def _(step):
            body(pl.ds(pl.multiple_of(start + step * BLOCK, BLOCK), BLOCK))

    quarter = lines * cb

    def lay_factor(at, length, width, value):
        high, low_part = halves(value)
        for third, part in enumerate((high, low_part, high)):
            here = pl.ds(pl.multiple_of(third * length + at.start, BLOCK), BLOCK)
            factor[here, 0:width] = part

    def keep_expr(k, at, value):
        start = sum(forward_widths[:k])
        for turn in range(turns):
            origin, width = sum(backward_widths[:turn]), backward_widths[turn]
            lo, hi = max(start, origin), min(start + forward_widths[k], origin + width)
            if lo < hi:
                high, low_part = halves(value[:, lo - start : hi - start])
                for third, part in enumerate((high, low_part, high)):
                    expr_3[at, pl.ds(3 * origin + third * width + lo - origin, hi - lo)] = part

    def three_turn_cols(k):
        return pl.ds(3 * sum(backward_widths[:k]), 3 * backward_widths[k])

    def forward_product(k):
        width = forward_widths[k]

        def lay(at):
            value = bb[k][at, :]
            lay_factor(at, quarter, width, value)
            keep_expr(k, at, value)

        in_blocks(0, quarter, lay)
        if k < chunks - 1:

            @pl.loop(0, PLANE * rows // TALL)
            def _(step):
                tall = pl.ds(pl.multiple_of(step * TALL, TALL), TALL)
                cs[k][tall, :] = product(probs_3[tall, :], factor[0 : 3 * quarter, 0:width], ((1,), (0,)))

            for p in mates:
                pass_pred(k, p)
        else:
            for side, served in ((1 - row, (mates[0], mates[2])), (row, (mates[1],))):
                pair = pl.ds(pl.multiple_of(2 * side * rows, 2 * rows), 2 * rows)
                cs[k][pair, :] = product(probs_3[pair, :], factor[0 : 3 * quarter, 0:width], ((1,), (0,)))
                for p in served:
                    pass_pred(k, p)

    def pass_pred(k, p):
        send(cs[k].at[share(p)], cr[k].at[q], c_s.at[k], c_r.at[k, q], mate(p))

    def finish_pred(k):
        total = cs[k][share(q), :]
        for p in mates:
            arrived(cr[k].at[p], c_r.at[k, p])
            total = total + cr[k][p]
        pr[:, cols(k)] = total
        if k == 0:
            p0[q] = total[:, 0:head]
            for p in mates:
                send(p0.at[q], p0.at[q], p0_s, p0_r.at[q], mate(p))
        truth = tg[:, cols(k)]
        for at, value in enumerate((total * truth, total * total, truth * truth)):
            sacc[at] += lane_groups(value)
        kept = valid * total
        stats = by_slide(kept * truth) + by_slide(kept * total) + by_slide(valid * truth * truth)
        s1[q, 0 : 3 * slides, cols(k)] = jnp.concatenate(stats, axis=0)

    early = sum(forward_widths[:EARLY])
    parts = (pl.ds(0, early), pl.ds(early, genes - early))

    def sum_plane(at):
        for p in mates:
            send(s1.at[q, :, parts[at]], s1.at[q, :, parts[at]], s1_s, s1_r.at[at, q], mate(p))

    def sum_line(at):
        for p in mates:
            arrived(s1.at[p, :, parts[at]], s1_r.at[at, p])
        s2[z, :, parts[at]] = (s1[0, :, parts[at]] + s1[1, :, parts[at]]) + (s1[2, :, parts[at]] + s1[3, :, parts[at]])
        for o in others:
            send(s2.at[z, :, parts[at]], s2.at[z, :, parts[at]], s2_s, s2_r.at[at, z], (o * PLANE + q, core))

    kept = {}

    def finish_genes(at):
        for o in others:
            arrived(s2.at[o, :, parts[at]], s2_r.at[at, o])
        total = s2[0, :, parts[at]]
        for line in range(1, lines):
            total = total + s2[line, :, parts[at]]
        gene_dot, gene_pred, gene_true = total[0:2], total[2:4], total[4:6]
        gene_inv = lax.rsqrt(gene_pred * gene_true + tiny)
        cos_gene = gene_dot * gene_inv
        gv[0:2, parts[at]] = gene_inv
        gv[2:4, parts[at]] = cos_gene * gene_true / (gene_pred * gene_true + tiny)
        kept["genes", at] = jnp.sum(jnp.sum(cos_gene, axis=1, keepdims=True), axis=0, keepdims=True)
        if at == 0:
            kept["mass"] = jnp.where(first, total[6:7, 0:1], total[6:7, 1:2])
            kept["cells"] = jnp.where(first, total[6:7, 2:3], total[6:7, 3:4])

    def sum_cores():
        sums = [jnp.sum(sacc[at], axis=1, keepdims=True) for at in range(3)]
        ss[core] = jnp.where(wide == 0, sums[0], jnp.where(wide == 1, sums[1], sums[2])).T[0:8]
        send(ss.at[core], ss.at[core], ss_s, ss_r, sibling)

    def finish_spots():
        lane_id = lax.broadcasted_iota(jnp.int32, (1, rows), 1)
        first_lane = lane_id < slide_rows
        lane_position = place * slide_rows + jnp.where(first_lane, lane_id, lane_id - slide_rows)
        lane_valid = (lane_position < jnp.where(first_lane, count_ref[0], count_ref[1])).astype(F32)
        arrived(ss.at[1 - core], ss_r)
        spot = ss[0] + ss[1]
        spot_dot, spot_pred, spot_true = spot[0:1], spot[1:2], spot[2:3]
        spot_inv = lax.rsqrt(spot_pred * spot_true + tiny)
        cos_spot = spot_dot * spot_inv
        spot_back = cos_spot * spot_true / (spot_pred * spot_true + tiny)
        kept["cos"] = jnp.sum(lane_valid * cos_spot, axis=1, keepdims=True)
        vectors = [lane_valid * spot_inv, lane_valid * spot_back, lane_valid, jnp.zeros((5, rows), F32)]
        vr[q] = jnp.concatenate(vectors, axis=0)
        sacc[0] = jnp.zeros_like(sacc[0])

    def gradient(truth, guess, by_row, k):
        pieces = []
        for m in range(slides):
            lo, hi = m * slide_rows, (m + 1) * slide_rows
            inverse, back = gv[m : m + 1, turn_cols(k)], gv[2 + m : 3 + m, turn_cols(k)]
            spot_inv, spot_back, spot_valid = by_row[lo:hi, 0:1], by_row[lo:hi, 1:2], by_row[lo:hi, 2:3]
            pieces.append(
                guess[lo:hi] * (spot_valid * back + spot_back) - truth[lo:hi] * (spot_valid * inverse + spot_inv)
            )
        return jnp.concatenate(pieces, axis=0)

    def head_gradient():
        for p in mates:
            arrived(t0.at[p], t0_r.at[p])
            arrived(p0.at[p], p0_r.at[p])
            arrived(vr.at[p], vr_r.at[p])
        for p in range(PLANE):
            ds[0][share(p), :] = gradient(t0[p], p0[p], vr[p].T, 0)
        sacc[0] += lane_groups(ds[0][share(q), :] * p0[q])

    def send_grad(k):
        if k == 0:
            for p in mates:
                send(vr.at[q], vr.at[q], vr_s, vr_r.at[q], mate(p))
            kept["by_row"] = vr[q].T
            return
        grad = gradient(tg[:, turn_cols(k)], pr[:, turn_cols(k)], kept["by_row"], k)
        here = ds[k].at[share(q)]
        here[...] = grad
        for p in mates:
            send(here, here, d_s.at[k], d_r.at[k, q], mate(p))
        sacc[0] += lane_groups(grad * pr[:, turn_cols(k)])

    def send_terms():
        mass_total, cell_total = kept["mass"], kept["cells"]
        portion = kcell / cell_total
        kl_rows = portion * (jnp.log(counted) - jnp.log(cell_total) - jnp.log(mass) + jnp.log(mass_total))
        dmass = scale_count * valid * (1.0 / mass_total - portion / mass)
        terms = jnp.sum(scale_count * kl_rows, axis=0, keepdims=True) - kept["cos"]
        l1[q] = jnp.broadcast_to(terms, (8, LANES))
        for p in mates:
            send(l1.at[q], l1.at[q], l1_s, l1_r.at[q], mate(p))
        inner = jnp.sum(sacc[0], axis=1, keepdims=True)
        inn[core] = jnp.where(wide == 0, inner, kept["genes", 0] + kept["genes", 1])
        send(inn.at[core], inn.at[core], in_s, in_r, sibling)
        rowv[1] = jnp.broadcast_to(dmass, (rows, LANES))

    middle = lines // 2

    def backward_product(k):
        if k == 0:
            head_gradient()
        else:
            for p in mates:
                arrived(ds[k].at[share(p)], d_r.at[k, p])
        width, spots = backward_widths[k], PLANE * rows

        def lay(at):
            value = ds[k][at, :]
            lay_factor(at, spots, width, value)
            grad_3[at, three_turn_cols(k)] = threefold(value)

        in_blocks(0, spots, lay)
        if not halved(k):

            @pl.loop(0, quarter // TALL)
            def _(step):
                tall = pl.ds(pl.multiple_of(step * TALL, TALL), TALL)
                es[k][tall, :] = product(turned_3[tall, :], factor[0 : 3 * spots, 0:width], ((1,), (0,)))

        for turn in range(2):
            if halved(k):
                side = (1 - z // middle) if turn == 0 else z // middle
                pair = pl.ds(pl.multiple_of(side * middle * cb, middle * cb), middle * cb)
                es[k][pair, :] = product(turned_3[pair, :], factor[0 : 3 * spots, 0:width], ((1,), (0,)))

            @pl.when(z == 0)
            def _():
                if halved(k):
                    pass_up(k, middle if turn == 0 else 1, middle if turn == 0 else middle - 1, turn)
                elif whole(k):
                    if turn == 0:
                        pass_up(k, 1, last, 0)
                elif turn == 0:
                    for line in range(last, 0, -1):
                        pass_up(k, line, 1, line)

            @pl.when(z == last)
            def _():
                if halved(k):
                    pass_down(k, 0 if turn == 0 else middle, middle if turn == 0 else middle - 1, turn)
                elif whole(k):
                    if turn == 0:
                        pass_down(k, 0, last, 0)
                elif turn == 0:
                    for line in range(last):
                        pass_down(k, line, 1, line)

    def halved(k):
        return k == 0

    def whole(k):
        return 0 < k < turns - SPLIT

    def pass_up(k, line, count, slot):
        here = pl.ds(line * cb, count * cb)
        send(es[k].at[here], ru[k].at[here], ru_s.at[k], ru_r.at[k, slot], up)

    def pass_down(k, line, count, slot):
        here = pl.ds(line * cb, count * cb)
        send(es[k].at[here], rd[k].at[here], rd_s.at[k], rd_r.at[k, slot], down)

    def take_up(k, line, count, slot):
        arrived(ru[k].at[pl.ds(line * cb, count * cb)], ru_r.at[k, slot])

    def take_down(k, line, count, slot):
        arrived(rd[k].at[pl.ds(line * cb, count * cb)], rd_r.at[k, slot])

    def add_up(k, line, count):
        def add(at):
            es[k][at, :] += ru[k][at, :]

        in_blocks(line * cb, count * cb, add)

    def add_down(k, line, count):
        def add(at):
            es[k][at, :] += rd[k][at, :]

        in_blocks(line * cb, count * cb, add)

    def rising(k, at):
        if halved(k) or whole(k):
            start = middle if halved(k) else at
            take_up(k, start, lines - start, 0)
            above = max(at + 1, start)
            add_up(k, above, lines - above)
            pass_up(k, above, lines - above, 0)
        else:
            for line in range(last, at, -1):
                take_up(k, line, 1, line)
                add_up(k, line, 1)
                pass_up(k, line, 1, line)

    def falling(k, at):
        if halved(k) or whole(k):
            end = middle if halved(k) else at + 1
            take_down(k, 0, end, 0)
            below = min(at, end)
            add_down(k, 0, below)
            pass_down(k, 0, below, 0)
        else:
            for line in range(at):
                take_down(k, line, 1, line)
                add_down(k, line, 1)
                pass_down(k, line, 1, line)

    def add_near(k):
        for at in range(1, last):

            @pl.when(z == at)
            def _():
                (rising if low(at) else falling)(k, at)

    def add_far(k):
        for at in range(1, last):

            @pl.when(z == at)
            def _():
                (falling if low(at) else rising)(k, at)

    def finish_expr(k):
        for at in range(lines):

            @pl.when(z == at)
            def _():
                if at > 0:
                    if halved(k) and at < middle:
                        take_up(k, at, 1, 1)
                    elif at == last and (halved(k) or whole(k)):
                        take_up(k, at, 1, 0)
                    elif not halved(k) and not whole(k):
                        take_up(k, at, 1, at)
                if at < last:
                    if halved(k) and at >= middle:
                        take_down(k, at, 1, 1)
                    elif at == 0 and (halved(k) or whole(k)):
                        take_down(k, at, 1, 0)
                    elif not halved(k) and not whole(k):
                        take_down(k, at, 1, at)

        from_low, from_high = z > 0, z < last

        @pl.loop(0, cb // BLOCK)
        def _(step):
            here = pl.ds(pl.multiple_of(step * BLOCK, BLOCK), BLOCK)
            own = pl.ds(pl.multiple_of(z * cb + step * BLOCK, BLOCK), BLOCK)
            total = es[k][own, :]
            total = total + jnp.where(from_low, ru[k][own, :], 0.0)
            ge[here, turn_cols(k)] = total + jnp.where(from_high, rd[k][own, :], 0.0)

    def probs_gradient(k):
        at = three_turn_cols(k)

        @pl.loop(0, PLANE * rows // TALL)
        def _(step):
            tall = pl.ds(pl.multiple_of(step * TALL, TALL), TALL)
            part = product(grad_3[tall, at], expr_3[:, at], ((1,), (1,)))
            if k == 0:
                fs[tall, :] = part
            else:
                fs[tall, :] += part

    def slide_of(p, m):
        return pl.ds(pl.multiple_of(p * rows + m * slide_rows, slide_rows), slide_rows)

    def sum_probs_cores():
        for p in mates + (q,):
            fx[p] = fs[slide_of(p, 1 - core), :]
            send(fx.at[p], fy.at[p], fx_s, fx_r.at[p], sibling)

    def return_probs():
        for p in mates:
            arrived(fy.at[p], fx_r.at[p])
            fz[p] = fs[slide_of(p, core), :] + fy[p]
            send(fz.at[p], fr.at[q], f_s, f_r.at[q], mate(p))
        arrived(fy.at[q], fx_r.at[q])
        fr[q] = fs[slide_of(q, core), :] + fy[q]

    def pass_terms():
        for p in mates:
            arrived(l1.at[p], l1_r.at[p])
        l2[z] = (l1[0] + l1[1]) + (l1[2] + l1[3])
        for o in others:
            send(l2.at[z], l2.at[z], l2_s, l2_r.at[z], (o * PLANE + q, core))

    def part_of(slide, m):
        start = slide * slide_rows + m * (slide_rows // 2)
        return pl.ds(pl.multiple_of(start, slide_rows // 2), slide_rows // 2)

    def finish_logits():
        arrived(inn.at[1 - core], in_r)
        rowv[2] = (inn[0] + inn[1]) + rowv[1] * rowv[0]
        for p in mates:
            arrived(fr.at[p], f_r.at[p])
        for m in range(2):

            @pl.loop(0, slide_rows // STEP_ROWS // 2)
            def _(step):
                row_at = (m * (slide_rows // STEP_ROWS // 2) + step) * STEP_ROWS
                at = pl.ds(pl.multiple_of(row_at, STEP_ROWS), STEP_ROWS)
                whole_at = pl.ds(pl.multiple_of(core * slide_rows + row_at, STEP_ROWS), STEP_ROWS)
                by_mass, total_inner = rowv[1, whole_at, 0:1], rowv[2, whole_at, 0:1]
                for p in range(PLANE):
                    for line in range(lines):
                        here, there = pl.ds(line * cb, cb), (line * PLANE + p) * cb
                        grad = fr[p, at, here] + by_mass * weights[:, there : there + cb]
                        glog[whole_at, pl.ds(there, cb)] = pq[p, whole_at, here] * (grad - total_inner)

            here = part_of(core, m)
            send(glog.at[here], glog.at[here], go_s, go_r.at[m], sibling)

    def forward_left():
        for k in range(chunks):

            @pl.when(z < last)
            def _():
                sent(bb[k].at[block(z)], ou_s.at[k])

            @pl.when(z > 0)
            def _():
                sent(bb[k].at[block(z)], od_s.at[k])

            for at in range(1, last):

                @pl.when(z == at)
                def _():
                    sent(bb[k].at[pl.ds(0, at * cb)], fu_s.at[k])
                    sent(bb[k].at[pl.ds((at + 1) * cb, (last - at) * cb)], fd_s.at[k])

        three = pl.ds(0, len(mates))
        sent(ab.at[three, half(0)], a_s)
        sent(ab.at[three, half(0)], a2_s)
        sent(rs.at[three], r_s)
        sent(t0.at[three], t0_s)
        sent(p0.at[three], p0_s)
        for k in range(chunks):
            sent(cr[k].at[three], c_s.at[k])
        sent(s1.at[three], s1_s)
        sent(s2.at[pl.ds(0, last)], s2_s)
        sent(ss.at[0], ss_s)

    steps = {
        "far": forward_far,
        "near": forward_near,
        "share": share_logits,
        "take": take_probs,
        "whole": gathered,
        "product": forward_product,
        "sum": finish_pred,
        "turn": transpose,
        "plane": sum_plane,
        "line": sum_line,
        "genes": finish_genes,
        "cores": sum_cores,
        "spots": finish_spots,
        "grad": send_grad,
        "terms": send_terms,
        "backward": backward_product,
        "probs": probs_gradient,
        "exchange": sum_probs_cores,
        "return": return_probs,
        "loss": pass_terms,
        "logits": finish_logits,
        "add_near": add_near,
        "add_far": add_far,
        "expr": finish_expr,
        "left": forward_left,
    }
    for name, *where in STEPS:
        steps[name](*where)

    for o in others:
        arrived(l2.at[o], l2_r.at[o])
    loss = l2[0]
    for line in range(1, lines):
        loss = loss + l2[line]
    loss_ref[...] = loss[0:1, 0:1] - (inn[0, 0:1, 1:2] + inn[1, 0:1, 1:2])
    for m in range(2):
        arrived(glog.at[part_of(1 - core, m)], go_r.at[m])

    for k in range(turns):
        for at in range(lines):

            @pl.when(z == at)
            def _():
                if at < last:
                    sent(es[k].at[pl.ds((at + 1) * cb, (last - at) * cb)], ru_s.at[k])
                if at > 0:
                    sent(es[k].at[pl.ds(0, at * cb)], rd_s.at[k])

    three = pl.ds(0, len(mates))
    for k in range(1, turns):
        sent(ds[k].at[pl.ds(0, len(mates) * rows)], d_s.at[k])
    sent(vr.at[three], vr_s)
    sent(inn.at[0], in_s)
    sent(l1.at[three], l1_s)
    sent(l2.at[pl.ds(0, last)], l2_s)
    sent(fr.at[three], f_s)
    sent(fx, fx_s)
    sent(glog.at[half(0)], go_s)


def lane_groups(value):
    parts = [value[:, at : at + LANES] for at in range(0, value.shape[1], LANES)]
    return functools.reduce(lambda a, b: a + b, parts)


def grouped(refs, sizes):
    at = 0
    for size in sizes:
        yield refs[at : at + size]
        at += size


def deliver(pred_in, loss_in, glog_in, gexp_in, pred_ref, loss_ref, glog_ref, gexp_ref, sems):
    slides, slide_rows = pred_ref.shape[0], pred_ref.shape[1]
    pairs = [(gexp_in, gexp_ref), (loss_in, loss_ref)]
    for m in range(slides):
        part = pl.ds(m * slide_rows, slide_rows)
        pairs += [(glog_in.at[part], glog_ref.at[m]), (pred_in.at[part], pred_ref.at[m])]
    copies = [pltpu.make_async_copy(src, dst, sems.at[at]) for at, (src, dst) in enumerate(pairs)]
    for copy in copies:
        copy.start()
    for copy in copies:
        copy.wait()


def plane_call(logits, expr, spatial, slide_spots, spot_cells, cell_prior, lines):
    slides, slide_rows, cells = logits.shape
    rows = slides * slide_rows
    cb, genes = expr.shape
    quarter = lines * cb
    spots = PLANE * rows
    chunks, turns = len(FORWARD), len(BACKWARD)
    dma = pltpu.SemaphoreType.DMA
    vmem = pltpu.VMEM
    anywhere = pl.BlockSpec(memory_space=pl.ANY)
    in_vmem = pl.BlockSpec(memory_space=pltpu.VMEM)
    scratch = [
        pltpu.SMEM((slides,), jnp.int32),
        vmem((slides, slide_rows), jnp.int32),
        vmem((1, cells), jnp.int32),
        vmem((rows, cells), F32),
        vmem((PLANE, slide_rows, quarter), F32),
        vmem((rows, genes), F32),
        vmem((cb, genes), F32),
        vmem((PLANE, rows, quarter), F32),
        vmem((PLANE, rows, quarter), F32),
        vmem((PLANE, rows, quarter), F32),
        vmem((spots, 3 * quarter), BF16),
        vmem((quarter, 3 * spots), BF16),
        vmem((quarter, 3 * genes), BF16),
        vmem((3, rows, LANES), F32),
        vmem((PLANE, 8, genes), F32),
        vmem((lines, 8, genes), F32),
        vmem((8, genes), F32),
        vmem((2, 8, rows), F32),
        vmem((3, rows, LANES), F32),
        vmem((PLANE, 8, rows), F32),
        vmem((spots, 3 * genes), BF16),
        vmem((3 * max(quarter, spots), max(FORWARD + BACKWARD)), BF16),
        vmem((PLANE, rows, BACKWARD[0]), F32),
        vmem((PLANE, rows, BACKWARD[0]), F32),
        vmem((PLANE, 8, rows), F32),
        vmem((spots, quarter), F32),
        vmem((PLANE, slide_rows, quarter), F32),
        vmem((PLANE, slide_rows, quarter), F32),
        vmem((PLANE, slide_rows, quarter), F32),
        vmem((PLANE, slide_rows, quarter), F32),
        vmem((2, rows, LANES), F32),
        vmem((PLANE, 8, LANES), F32),
        vmem((lines, 8, LANES), F32),
        dma((2 * slides + 4,)),
        dma((chunks,)),
        dma((chunks,)),
        dma((chunks,)),
        dma((chunks,)),
        dma((chunks,)),
        dma((chunks,)),
        dma((chunks,)),
        dma((chunks,)),
        dma,
        dma((PLANE,)),
        dma,
        dma((PLANE,)),
        dma,
        dma((PLANE,)),
        dma((chunks,)),
        dma((chunks, PLANE)),
        dma,
        dma((2, PLANE)),
        dma,
        dma((2, lines)),
        dma,
        dma,
        dma((turns,)),
        dma((turns, PLANE)),
        dma((turns,)),
        dma((turns, lines)),
        dma((turns,)),
        dma((turns, lines)),
        dma,
        dma((PLANE,)),
        dma,
        dma((PLANE,)),
        dma,
        dma((2,)),
        dma,
        dma,
        dma,
        dma((PLANE,)),
        dma,
        dma((lines,)),
        dma,
        dma((PLANE,)),
        dma,
        dma((PLANE,)),
        dma,
        dma((PLANE,)),
    ]
    for shape, widths in (
        ((quarter,), FORWARD),
        ((spots,), FORWARD),
        ((PLANE, rows), FORWARD),
        ((spots,), BACKWARD),
        ((quarter,), BACKWARD),
        ((quarter,), BACKWARD),
        ((quarter,), BACKWARD),
    ):
        scratch += [vmem(shape + (width,), F32) for width in widths]
    in_hbm = functools.partial(pltpu.with_memory_space_constraint, memory_space=pltpu.HBM)
    in_place = functools.partial(pltpu.with_memory_space_constraint, memory_space=pltpu.VMEM)
    results = pl.pallas_call(
        functools.partial(plane_kernel, lines, FORWARD, BACKWARD),
        out_shape=(
            vmem((rows, genes), F32),
            vmem((1, 1), F32),
            vmem((rows, cells), F32),
            vmem((cb, genes), F32),
        ),
        in_specs=[anywhere] * 6,
        out_specs=(in_vmem,) * 4,
        scratch_shapes=scratch,
        compiler_params=pltpu.CompilerParams(
            collective_id=0, has_side_effects=True, vmem_limit_bytes=48 * 1024 * 1024
        ),
    )(*map(in_hbm, (logits, expr, spatial, slide_spots, spot_cells, cell_prior.reshape(1, cells))))
    pred, loss, grad_logits, grad_expr = pl.pallas_call(
        deliver,
        out_shape=(
            jax.ShapeDtypeStruct((slides, slide_rows, genes), F32),
            jax.ShapeDtypeStruct((1, 1), F32),
            jax.ShapeDtypeStruct((slides, slide_rows, cells), F32),
            jax.ShapeDtypeStruct((cb, genes), F32),
        ),
        in_specs=[anywhere] * 4,
        out_specs=(anywhere,) * 4,
        scratch_shapes=[dma((2 * slides + 2,))],
        compiler_params=pltpu.CompilerParams(vmem_limit_bytes=4 * 1024 * 1024),
    )(*map(in_place, results))
    return pred, loss.reshape(()), grad_logits, grad_expr


def general_plan(logits, expr, spatial, slide_spots, spot_cells, cell_prior):
    place = lax.axis_index("spot")
    side = lax.axis_index("gene")
    rows_all = logits.shape[1]
    cell_rows = expr.shape[0]
    weights = cell_prior.astype(jnp.float32) / fixed_point
    gene_share = (place == 0).astype(jnp.float32)
    row_share = (side == 0).astype(jnp.float32)
    own_weights = lax.dynamic_slice_in_dim(weights, place * cell_rows, cell_rows, 0)
    expr_acc = jnp.zeros((cell_rows, expr.shape[1]), jnp.float32)
    loss_local = jnp.zeros((), jnp.float32)
    pred_list = []
    grad_list = []
    for slide in range(logits.shape[0]):
        logit_rows = logits[slide]
        counted = spot_cells[slide].astype(jnp.float32)
        target = spatial[slide]
        positions = place * rows_all + jnp.arange(rows_all, dtype=jnp.int32)
        valid = (positions < slide_spots[slide]).astype(jnp.float32)
        peak = jnp.max(logit_rows, axis=1, keepdims=True)
        raised = jnp.exp(logit_rows - peak)
        probs = raised / jnp.sum(raised, axis=1, keepdims=True)
        mass = jnp.dot(probs, weights, precision=lax.Precision.HIGHEST)
        blocks = lax.all_to_all(probs, "spot", split_axis=1, concat_axis=0, tiled=True)
        pred = lax.psum_scatter(
            jnp.dot(blocks, expr, precision=lax.Precision.HIGHEST),
            "spot",
            scatter_dimension=0,
            tiled=True,
        )
        gene_dot = jnp.sum(valid[:, None] * pred * target, axis=0)
        gene_pred = jnp.sum(valid[:, None] * pred * pred, axis=0)
        gene_true = jnp.sum(valid[:, None] * target * target, axis=0)
        mass_part = jnp.sum(valid * mass)
        kcell = valid * counted
        cell_part = jnp.sum(kcell)
        spot_dot = jnp.sum(pred * target, axis=1)
        spot_pred = jnp.sum(pred * pred, axis=1)
        spot_true = jnp.sum(target * target, axis=1)
        gene_dot, gene_pred, gene_true, mass_total, cell_total = lax.psum(
            (gene_dot, gene_pred, gene_true, mass_part, cell_part), "spot"
        )
        spot_dot, spot_pred, spot_true = lax.psum((spot_dot, spot_pred, spot_true), "gene")
        gene_inv = lax.rsqrt(gene_pred * gene_true + tiny)
        cos_gene = gene_dot * gene_inv
        spot_inv = lax.rsqrt(spot_pred * spot_true + tiny)
        cos_spot = spot_dot * spot_inv
        share = kcell / cell_total
        scale_count = slide_spots[slide].astype(jnp.float32)
        kl_part = jnp.sum(
            share * (jnp.log(counted) - jnp.log(cell_total) - jnp.log(mass) + jnp.log(mass_total))
        )
        loss_local = loss_local - gene_share * jnp.sum(cos_gene)
        loss_local = loss_local + row_share * (scale_count * kl_part - jnp.sum(valid * cos_spot))
        gene_back = cos_gene * gene_true / (gene_pred * gene_true + tiny)
        spot_back = cos_spot * spot_true / (spot_pred * spot_true + tiny)
        dpred = -valid[:, None] * (
            target * (gene_inv[None, :] + spot_inv[:, None])
            - pred * gene_back[None, :]
            - pred * spot_back[:, None]
        )
        dmass = scale_count * valid * (1.0 / mass_total - share / mass)
        pred_list.append(pred)
        grads_full, mass_full = (
            lax.all_gather(dpred, "spot", axis=0, tiled=True),
            lax.all_gather(dmass, "spot", axis=0, tiled=True),
        )
        dprob_cells = jnp.dot(grads_full, expr.T, precision=lax.Precision.HIGHEST)
        dprob_cells = lax.psum(dprob_cells, "gene")
        expr_acc = expr_acc + lax.dot_general(
            blocks, grads_full, (((0,), (0,)), ((), ())), precision=lax.Precision.HIGHEST
        )
        dprob_cells = dprob_cells + mass_full[:, None] * own_weights[None, :]
        dprob_rows = lax.all_to_all(dprob_cells, "spot", split_axis=0, concat_axis=1, tiled=True)
        inner = jnp.sum(probs * dprob_rows, axis=1, keepdims=True)
        dlogit = probs * (dprob_rows - inner)
        grad_list.append(dlogit)
    loss = lax.psum(loss_local, ("spot", "gene"))
    return (jnp.stack(pred_list), loss, jnp.stack(grad_list), expr_acc)


def solution(mesh):
    places = mesh.shape["spot"]

    def on_device(logits, expr, spatial, slide_spots, spot_cells, cell_prior):
        if places == PLANE * PLANE and mesh.shape["gene"] == 2 and expr.shape[1] == sum(FORWARD):
            return plane_call(
                logits, expr, spatial, slide_spots, spot_cells, cell_prior, places // PLANE
            )
        return general_plan(logits, expr, spatial, slide_spots, spot_cells, cell_prior)

    in_specs = (
        P(None, "spot", None),
        P("spot", "gene"),
        P(None, "spot", "gene"),
        P(),
        P(None, "spot"),
        P(),
    )
    out_specs = (P(None, "spot", "gene"), P(), P(None, "spot", None), P("spot", "gene"))
    return jax.shard_map(
        on_device, mesh=mesh, in_specs=in_specs, out_specs=out_specs, check_vma=False
    )
```

```python
import functools

import jax
import jax.numpy as jnp
from jax import lax
from jax.experimental import pallas as pl
from jax.experimental.pallas import tpu as pltpu
from jax.sharding import PartitionSpec as P

tiny = 1e-06
fixed_point = 16384.0
F32 = jnp.float32
BF16 = jnp.bfloat16
MESH = pl.DeviceIdType.MESH

PLANE = 4
LANES = 128
STEP_ROWS = 16
BLOCK = 32
TALL = 256
FORWARD = (128, 256, 256, 128, 128, 128)
BACKWARD = (128, 128, 256, 256, 256)
SPLIT = 4
LEAD = 1
NEAR_LEAD = 3
EARLY = 3
STEPS = (
    ("far", 0),
    ("far", 1),
    ("next", 0),
    ("near", 0),
    ("share",),
    ("next", 1),
    ("far", 2),
    ("far", 3),
    ("take",),
    ("whole", 0),
    ("near", 1),
    ("next", 2),
    ("product", 0),
    ("sum", 0),
    ("whole", 1),
    ("near", 2),
    ("next", 3),
    ("product", 1),
    ("whole", 2),
    ("product", 2),
    ("whole", 3),
    ("near", 3),
    ("next", 4),
    ("product", 3),
    ("far", 4),
    ("whole", 4),
    ("near", 4),
    ("next", 5),
    ("product", 4),
    ("sum", 1),
    ("turn", 0),
    ("far", 5),
    ("whole", 5),
    ("near", 5),
    ("product", 5),
    ("sum", 2),
    ("plane", 0),
    ("turn", 1),
    ("sum", 3),
    ("line", 0),
    ("sum", 4),
    ("sum", 5),
    ("plane", 1),
    ("cores",),
    ("genes", 0),
    ("spots",),
    ("grad", 0),
    ("grad", 1),
    ("grad", 2),
    ("line", 1),
    ("backward", 0),
    ("backward", 1),
    ("add_near", 0),
    ("genes", 1),
    ("grad", 3),
    ("backward", 2),
    ("probs", 0),
    ("add_far", 0),
    ("probs", 1),
    ("expr", 0),
    ("grad", 4),
    ("add_near", 1),
    ("probs", 2),
    ("terms",),
    ("backward", 3),
    ("probs", 3),
    ("add_near", 2),
    ("backward", 4),
    ("add_far", 1),
    ("probs", 4),
    ("exchange",),
    ("add_near", 3),
    ("add_far", 2),
    ("left",),
    ("return",),
    ("loss",),
    ("add_far", 3),
    ("expr", 1),
    ("add_near", 4),
    ("logits",),
    ("add_far", 4),
    ("expr", 2),
    ("expr", 3),
    ("expr", 4),
)


def halves(value):
    high = value.astype(BF16)
    return high, (value - high.astype(F32)).astype(BF16)


def threefold(value):
    high, low = halves(value)
    return jnp.concatenate([high, high, low], axis=1)


def product(a, b, contract):
    return lax.dot_general(a, b, (contract, ((), ())), preferred_element_type=F32)


def plane_kernel(lines, forward_widths, backward_widths, *refs):
    chunks, turns = len(forward_widths), len(backward_widths)
    (
        (logits_ref, expr_ref, spatial_ref, count_in, cells_in, prior_in),
        (pr, loss_ref, glog, ge),
        (count_ref, cells_ref, prior_ref, lg, lq, tg, ex, pq, ab, af, probs_3, turned_3, expr_3, sacc, s1, s2, gv, ss, rowv, rs),
        (grad_3, factor, t0, p0, vr, fs, fx, fy, fz, fr, inn, l1, l2),
        (loc, ou_s, ou_r, od_s, od_r, fu_s, fu_r, fd_s, fd_r, a_s, a_r, a2_s, a2_r, r_s, r_r),
        (c_s, c_r, s1_s, s1_r, s2_s, s2_r, ss_s, ss_r, d_s, d_r, ru_s, ru_r, rd_s, rd_r),
        (f_s, f_r, fx_s, fx_r, go_s, go_r, in_s, in_r, l1_s, l1_r, l2_s, l2_r, t0_s, t0_r, p0_s, p0_r, vr_s, vr_r),
        bb,
        cs,
        cr,
        ds,
        es,
        ru,
        rd,
    ) = grouped(refs, (6, 4, 20, 13, 15, 14, 18, chunks, chunks, chunks, turns, turns, turns, turns))
    place = lax.axis_index("spot")
    core = lax.axis_index("gene")
    z = place // PLANE
    q = place % PLANE
    col, row = q % 2, q // 2
    mates = ((1 - row) * 2 + 1 - col, row * 2 + 1 - col, (1 - row) * 2 + col)
    others = tuple((z + step) % lines for step in range(1, lines))
    up, down = (place + PLANE, core), (place - PLANE, core)
    sibling = (place, 1 - core)
    slides, slide_rows = logits_ref.shape[0], logits_ref.shape[1]
    rows = slides * slide_rows
    cb = expr_ref.shape[0]
    genes = expr_ref.shape[1]
    last = lines - 1

    def mate(p):
        return (z * PLANE + p, core)

    def send(src, dst, send_sem, recv_sem, device):
        copy = pltpu.make_async_remote_copy(
            src_ref=src, dst_ref=dst, send_sem=send_sem, recv_sem=recv_sem, device_id=device, device_id_type=MESH
        )
        copy.start()

    def arrived(dst, recv_sem):
        pltpu.make_async_copy(dst, dst, recv_sem).wait()

    sent = arrived

    def cols(k):
        return pl.ds(sum(forward_widths[:k]), forward_widths[k])

    def turn_cols(k):
        return pl.ds(sum(backward_widths[:k]), backward_widths[k])

    def block(index):
        return pl.ds(pl.multiple_of(index * cb, cb), cb)

    def share(index):
        return pl.ds(pl.multiple_of(index * rows, rows), rows)

    def half(index):
        return pl.ds(pl.multiple_of(index * slide_rows, slide_rows), slide_rows)

    small = ((prior_in, prior_ref), (count_in, count_ref), (cells_in, cells_ref))
    pltpu.make_async_copy(expr_ref, ex, loc.at[2 * slides]).start()
    for m in range(slides):
        pltpu.make_async_copy(logits_ref.at[m], lg.at[half(m)], loc.at[m]).start()
    for at, (src, dst) in enumerate(small):
        pltpu.make_async_copy(src, dst, loc.at[2 * slides + 1 + at]).start()
    for m in range(slides):
        pltpu.make_async_copy(spatial_ref.at[m], tg.at[half(m)], loc.at[slides + m]).start()

    barrier = pltpu.get_barrier_semaphore()
    for p in mates:
        pl.semaphore_signal(barrier, inc=1, device_id=mate(p), device_id_type=MESH)
    for o in others:
        pl.semaphore_signal(barrier, inc=1, device_id=(o * PLANE + q, core), device_id_type=MESH)
    pl.semaphore_signal(barrier, inc=1, device_id=sibling, device_id_type=MESH)
    pltpu.make_async_copy(expr_ref, ex, loc.at[2 * slides]).wait()
    for k in range(chunks):
        bb[k][block(z), :] = ex[:, cols(k)]
    for m in range(slides):
        pltpu.make_async_copy(logits_ref.at[m], lg.at[half(m)], loc.at[m]).wait()
    for p in range(PLANE):
        for line in range(lines):
            lq[p, :, pl.ds(line * cb, cb)] = lg[half(core), pl.ds((line * PLANE + p) * cb, cb)]
    pl.semaphore_wait(barrier, len(mates) + len(others) + 1)

    def own_up(k):
        here = bb[k].at[block(z)]
        send(here, here, ou_s.at[k], ou_r.at[k], up)

    def own_down(k):
        here = bb[k].at[block(z)]
        send(here, here, od_s.at[k], od_r.at[k], down)

    def low(at):
        return 2 * at < lines

    for at in range(lines):

        @pl.when(z == at)
        def _():
            for k in range(chunks):
                if at < last and (at == 0 or k < (LEAD if low(at) else NEAR_LEAD)):
                    own_up(k)
                if at > 0 and (at == last or k < (NEAR_LEAD if low(at) else LEAD)):
                    own_down(k)

    for p in mates:
        send(lq.at[p], ab.at[q, half(core)], a_s, a_r.at[q], mate(p))

    def come_up(k, at, line):
        arrived(bb[k].at[pl.ds(line * cb, cb)], ou_r.at[k] if line == at - 1 else fu_r.at[k, line])

    def come_down(k, at, line):
        arrived(bb[k].at[pl.ds(line * cb, cb)], od_r.at[k] if line == at + 1 else fd_r.at[k, line])

    def upward(k, at, blocks):
        for line in blocks:
            come_up(k, at, line)
            here = bb[k].at[pl.ds(line * cb, cb)]
            send(here, here, fu_s.at[k], fu_r.at[k, line], up)

    def downward(k, at, blocks):
        for line in blocks:
            come_down(k, at, line)
            here = bb[k].at[pl.ds(line * cb, cb)]
            send(here, here, fd_s.at[k], fd_r.at[k, line], down)

    def forward_far(k):
        for at in range(1, last):

            @pl.when(z == at)
            def _():
                if low(at):
                    upward(k, at, range(at - 1, -1, -1))
                else:
                    downward(k, at, range(at + 1, lines))
                if k + LEAD < chunks:
                    (own_up if low(at) else own_down)(k + LEAD)

    def forward_next(k):
        for at in range(1, last):

            @pl.when(z == at)
            def _():
                if low(at):
                    downward(k, at, (at + 1,))
                else:
                    upward(k, at, (at - 1,))

    def forward_near(k):
        for at in range(1, last):

            @pl.when(z == at)
            def _():
                if low(at):
                    downward(k, at, range(at + 2, lines))
                else:
                    upward(k, at, range(at - 2, -1, -1))
                if k + NEAR_LEAD < chunks:
                    (own_down if low(at) else own_up)(k + NEAR_LEAD)

    def gathered(k):
        @pl.when(z == 0)
        def _():
            for line in range(1, lines):
                come_down(k, 0, line)

        @pl.when(z == last)
        def _():
            for line in range(last):
                come_up(k, last, line)

    for at, (src, dst) in enumerate(small):
        pltpu.make_async_copy(src, dst, loc.at[2 * slides + 1 + at]).wait()
    weights = prior_ref[...].astype(F32) / fixed_point

    @pl.loop(0, rows // STEP_ROWS)
    def _(step):
        at = pl.ds(pl.multiple_of(step * STEP_ROWS, STEP_ROWS), STEP_ROWS)
        value = lg[at, :]
        peak = jnp.max(value, axis=1, keepdims=True)
        raised = jnp.exp(value - peak)
        scale = 1.0 / jnp.sum(raised, axis=1, keepdims=True)
        probs = raised * scale
        mass_rows = jnp.sum(probs * weights, axis=1, keepdims=True)
        rowv[0, at, :] = jnp.broadcast_to(mass_rows, (STEP_ROWS, LANES))
        rowv[1, at, :] = jnp.broadcast_to(peak, (STEP_ROWS, LANES))
        rowv[2, at, :] = jnp.broadcast_to(scale, (STEP_ROWS, LANES))
        for p in range(PLANE):
            for line in range(lines):
                at_cells = (line * PLANE + p) * cb
                pq[p, at, pl.ds(line * cb, cb)] = probs[:, at_cells : at_cells + cb]

    wide = lax.broadcasted_iota(jnp.int32, (rows, LANES), 1)
    rs[q] = jnp.where(wide == 0, rowv[1], rowv[2]).T[0:8]
    for p in mates:
        send(rs.at[q], rs.at[q], r_s, r_r.at[q], mate(p))

    rid = lax.broadcasted_iota(jnp.int32, (rows, 1), 0)
    first = rid < slide_rows
    position = place * slide_rows + jnp.where(first, rid, rid - slide_rows)
    count = jnp.where(first, count_ref[0], count_ref[1])
    valid = (position < count).astype(F32)
    scale_count = count.astype(F32)
    square = (slide_rows, slide_rows)
    eye = lax.broadcasted_iota(jnp.int32, square, 0) == lax.broadcasted_iota(jnp.int32, square, 1)
    counted = jnp.concatenate(
        [
            jnp.sum(jnp.where(eye, cells_ref[m : m + 1, :].astype(F32), 0.0), axis=1, keepdims=True)
            for m in range(slides)
        ],
        axis=0,
    )
    mass = rowv[0, :, 0:1]
    kcell = valid * counted

    def by_slide(value):
        return [jnp.sum(value[m * slide_rows : (m + 1) * slide_rows], axis=0, keepdims=True) for m in range(slides)]

    mass_parts = by_slide(valid * mass)
    cell_parts = by_slide(kcell)
    lane = lax.broadcasted_iota(jnp.int32, (1, LANES), 1)
    scalars = jnp.zeros((1, LANES), F32)
    for at, value in enumerate(mass_parts + cell_parts):
        scalars = jnp.where(lane == at, value, scalars)
    for m in range(slides):
        pltpu.make_async_copy(spatial_ref.at[m], tg.at[half(m)], loc.at[slides + m]).wait()

    head = backward_widths[0]
    t0[q] = tg[:, 0:head]
    for p in mates:
        send(t0.at[q], t0.at[q], t0_s, t0_r.at[q], mate(p))
    sacc[...] = jnp.zeros_like(sacc)
    s1[q, 3 * slides :, :] = jnp.zeros((8 - 3 * slides, genes), F32)
    s1[q, 3 * slides : 3 * slides + 1, 0:LANES] = scalars

    def share_logits():
        for p in (mates[1], mates[2], mates[0]):
            here = ab.at[p, half(core)]
            arrived(here, a_r.at[p])
            send(here, here, a2_s, a2_r.at[p], sibling)

    def lay_probs(p, at, value):
        af[p, at, :] = value
        there = pl.ds(pl.multiple_of(p * rows + at.start, BLOCK), BLOCK)
        probs_3[there, :] = threefold(value)

    def take_probs():
        in_blocks(0, rows, lambda at: lay_probs(q, at, pq[q, at, :]))
        for p in (mates[1], mates[2], mates[0]):
            arrived(rs.at[p], r_r.at[p])
            arrived(ab.at[p, half(1 - core)], a2_r.at[p])
            rowv[1] = jnp.concatenate([rs[p].T, jnp.zeros((rows, LANES - 8), F32)], axis=1)

            def take(at):
                probs = jnp.exp(ab[p, at, :] - rowv[1, at, 0:1]) * rowv[1, at, 1:2]
                lay_probs(p, at, probs)

            in_blocks(0, rows, take)

    def transpose(part):
        @pl.loop(0, PLANE // 2)
        def _(step):
            p = part * (PLANE // 2) + step
            high, low_part = halves(af[p].T)
            for third, value in enumerate((high, high, low_part)):
                turned_3[:, pl.ds(pl.multiple_of(third * PLANE * rows + p * rows, rows), rows)] = value

    def in_blocks(start, count, body):
        @pl.loop(0, count // BLOCK)
        def _(step):
            body(pl.ds(pl.multiple_of(start + step * BLOCK, BLOCK), BLOCK))

    quarter = lines * cb

    def lay_factor(at, length, width, value):
        high, low_part = halves(value)
        for third, part in enumerate((high, low_part, high)):
            here = pl.ds(pl.multiple_of(third * length + at.start, BLOCK), BLOCK)
            factor[here, 0:width] = part

    def keep_expr(k, at, value):
        start = sum(forward_widths[:k])
        for turn in range(turns):
            origin, width = sum(backward_widths[:turn]), backward_widths[turn]
            lo, hi = max(start, origin), min(start + forward_widths[k], origin + width)
            if lo < hi:
                high, low_part = halves(value[:, lo - start : hi - start])
                for third, part in enumerate((high, low_part, high)):
                    expr_3[at, pl.ds(3 * origin + third * width + lo - origin, hi - lo)] = part

    def three_turn_cols(k):
        return pl.ds(3 * sum(backward_widths[:k]), 3 * backward_widths[k])

    def forward_product(k):
        width = forward_widths[k]

        def lay(at):
            value = bb[k][at, :]
            lay_factor(at, quarter, width, value)
            keep_expr(k, at, value)

        in_blocks(0, quarter, lay)
        if k < chunks - 1:

            @pl.loop(0, PLANE * rows // TALL)
            def _(step):
                tall = pl.ds(pl.multiple_of(step * TALL, TALL), TALL)
                cs[k][tall, :] = product(probs_3[tall, :], factor[0 : 3 * quarter, 0:width], ((1,), (0,)))

            for p in mates:
                pass_pred(k, p)
        else:
            for side, served in ((1 - row, (mates[0], mates[2])), (row, (mates[1],))):
                pair = pl.ds(pl.multiple_of(2 * side * rows, 2 * rows), 2 * rows)
                cs[k][pair, :] = product(probs_3[pair, :], factor[0 : 3 * quarter, 0:width], ((1,), (0,)))
                for p in served:
                    pass_pred(k, p)

    def pass_pred(k, p):
        send(cs[k].at[share(p)], cr[k].at[q], c_s.at[k], c_r.at[k, q], mate(p))

    def finish_pred(k):
        total = cs[k][share(q), :]
        for p in mates:
            arrived(cr[k].at[p], c_r.at[k, p])
            total = total + cr[k][p]
        pr[:, cols(k)] = total
        if k == 0:
            p0[q] = total[:, 0:head]
            for p in mates:
                send(p0.at[q], p0.at[q], p0_s, p0_r.at[q], mate(p))
        truth = tg[:, cols(k)]
        for at, value in enumerate((total * truth, total * total, truth * truth)):
            sacc[at] += lane_groups(value)
        kept = valid * total
        stats = by_slide(kept * truth) + by_slide(kept * total) + by_slide(valid * truth * truth)
        s1[q, 0 : 3 * slides, cols(k)] = jnp.concatenate(stats, axis=0)

    early = sum(forward_widths[:EARLY])
    parts = (pl.ds(0, early), pl.ds(early, genes - early))

    def sum_plane(at):
        for p in mates:
            send(s1.at[q, :, parts[at]], s1.at[q, :, parts[at]], s1_s, s1_r.at[at, q], mate(p))

    def sum_line(at):
        for p in mates:
            arrived(s1.at[p, :, parts[at]], s1_r.at[at, p])
        s2[z, :, parts[at]] = (s1[0, :, parts[at]] + s1[1, :, parts[at]]) + (s1[2, :, parts[at]] + s1[3, :, parts[at]])
        for o in others:
            send(s2.at[z, :, parts[at]], s2.at[z, :, parts[at]], s2_s, s2_r.at[at, z], (o * PLANE + q, core))

    kept = {}

    def finish_genes(at):
        for o in others:
            arrived(s2.at[o, :, parts[at]], s2_r.at[at, o])
        total = s2[0, :, parts[at]]
        for line in range(1, lines):
            total = total + s2[line, :, parts[at]]
        gene_dot, gene_pred, gene_true = total[0:2], total[2:4], total[4:6]
        gene_inv = lax.rsqrt(gene_pred * gene_true + tiny)
        cos_gene = gene_dot * gene_inv
        gv[0:2, parts[at]] = gene_inv
        gv[2:4, parts[at]] = cos_gene * gene_true / (gene_pred * gene_true + tiny)
        kept["genes", at] = jnp.sum(jnp.sum(cos_gene, axis=1, keepdims=True), axis=0, keepdims=True)
        if at == 0:
            kept["mass"] = jnp.where(first, total[6:7, 0:1], total[6:7, 1:2])
            kept["cells"] = jnp.where(first, total[6:7, 2:3], total[6:7, 3:4])

    def sum_cores():
        sums = [jnp.sum(sacc[at], axis=1, keepdims=True) for at in range(3)]
        ss[core] = jnp.where(wide == 0, sums[0], jnp.where(wide == 1, sums[1], sums[2])).T[0:8]
        send(ss.at[core], ss.at[core], ss_s, ss_r, sibling)

    def finish_spots():
        lane_id = lax.broadcasted_iota(jnp.int32, (1, rows), 1)
        first_lane = lane_id < slide_rows
        lane_position = place * slide_rows + jnp.where(first_lane, lane_id, lane_id - slide_rows)
        lane_valid = (lane_position < jnp.where(first_lane, count_ref[0], count_ref[1])).astype(F32)
        arrived(ss.at[1 - core], ss_r)
        spot = ss[0] + ss[1]
        spot_dot, spot_pred, spot_true = spot[0:1], spot[1:2], spot[2:3]
        spot_inv = lax.rsqrt(spot_pred * spot_true + tiny)
        cos_spot = spot_dot * spot_inv
        spot_back = cos_spot * spot_true / (spot_pred * spot_true + tiny)
        kept["cos"] = jnp.sum(lane_valid * cos_spot, axis=1, keepdims=True)
        vectors = [lane_valid * spot_inv, lane_valid * spot_back, lane_valid, jnp.zeros((5, rows), F32)]
        vr[q] = jnp.concatenate(vectors, axis=0)
        sacc[0] = jnp.zeros_like(sacc[0])

    def gradient(truth, guess, by_row, k):
        pieces = []
        for m in range(slides):
            lo, hi = m * slide_rows, (m + 1) * slide_rows
            inverse, back = gv[m : m + 1, turn_cols(k)], gv[2 + m : 3 + m, turn_cols(k)]
            spot_inv, spot_back, spot_valid = by_row[lo:hi, 0:1], by_row[lo:hi, 1:2], by_row[lo:hi, 2:3]
            pieces.append(
                guess[lo:hi] * (spot_valid * back + spot_back) - truth[lo:hi] * (spot_valid * inverse + spot_inv)
            )
        return jnp.concatenate(pieces, axis=0)

    def head_gradient():
        for p in mates:
            arrived(t0.at[p], t0_r.at[p])
            arrived(p0.at[p], p0_r.at[p])
            arrived(vr.at[p], vr_r.at[p])
        for p in range(PLANE):
            ds[0][share(p), :] = gradient(t0[p], p0[p], vr[p].T, 0)
        sacc[0] += lane_groups(ds[0][share(q), :] * p0[q])

    def send_grad(k):
        if k == 0:
            for p in mates:
                send(vr.at[q], vr.at[q], vr_s, vr_r.at[q], mate(p))
            kept["by_row"] = vr[q].T
            return
        grad = gradient(tg[:, turn_cols(k)], pr[:, turn_cols(k)], kept["by_row"], k)
        here = ds[k].at[share(q)]
        here[...] = grad
        for p in mates:
            send(here, here, d_s.at[k], d_r.at[k, q], mate(p))
        sacc[0] += lane_groups(grad * pr[:, turn_cols(k)])

    def send_terms():
        mass_total, cell_total = kept["mass"], kept["cells"]
        portion = kcell / cell_total
        kl_rows = portion * (jnp.log(counted) - jnp.log(cell_total) - jnp.log(mass) + jnp.log(mass_total))
        dmass = scale_count * valid * (1.0 / mass_total - portion / mass)
        terms = jnp.sum(scale_count * kl_rows, axis=0, keepdims=True) - kept["cos"]
        l1[q] = jnp.broadcast_to(terms, (8, LANES))
        for p in mates:
            send(l1.at[q], l1.at[q], l1_s, l1_r.at[q], mate(p))
        inner = jnp.sum(sacc[0], axis=1, keepdims=True)
        inn[core] = jnp.where(wide == 0, inner, kept["genes", 0] + kept["genes", 1])
        send(inn.at[core], inn.at[core], in_s, in_r, sibling)
        rowv[1] = jnp.broadcast_to(dmass, (rows, LANES))

    middle = lines // 2

    def backward_product(k):
        if k == 0:
            head_gradient()
        else:
            for p in mates:
                arrived(ds[k].at[share(p)], d_r.at[k, p])
        width, spots = backward_widths[k], PLANE * rows

        def lay(at):
            value = ds[k][at, :]
            lay_factor(at, spots, width, value)
            grad_3[at, three_turn_cols(k)] = threefold(value)

        in_blocks(0, spots, lay)
        if not halved(k):

            @pl.loop(0, quarter // TALL)
            def _(step):
                tall = pl.ds(pl.multiple_of(step * TALL, TALL), TALL)
                es[k][tall, :] = product(turned_3[tall, :], factor[0 : 3 * spots, 0:width], ((1,), (0,)))

        for turn in range(2):
            if halved(k):
                side = (1 - z // middle) if turn == 0 else z // middle
                pair = pl.ds(pl.multiple_of(side * middle * cb, middle * cb), middle * cb)
                es[k][pair, :] = product(turned_3[pair, :], factor[0 : 3 * spots, 0:width], ((1,), (0,)))

            @pl.when(z == 0)
            def _():
                if halved(k):
                    pass_up(k, middle if turn == 0 else 1, middle if turn == 0 else middle - 1, turn)
                elif whole(k):
                    if turn == 0:
                        pass_up(k, 1, last, 0)
                elif turn == 0:
                    for line in range(last, 0, -1):
                        pass_up(k, line, 1, line)

            @pl.when(z == last)
            def _():
                if halved(k):
                    pass_down(k, 0 if turn == 0 else middle, middle if turn == 0 else middle - 1, turn)
                elif whole(k):
                    if turn == 0:
                        pass_down(k, 0, last, 0)
                elif turn == 0:
                    for line in range(last):
                        pass_down(k, line, 1, line)

    def halved(k):
        return k == 0

    def whole(k):
        return 0 < k < turns - SPLIT

    def pass_up(k, line, count, slot):
        here = pl.ds(line * cb, count * cb)
        send(es[k].at[here], ru[k].at[here], ru_s.at[k], ru_r.at[k, slot], up)

    def pass_down(k, line, count, slot):
        here = pl.ds(line * cb, count * cb)
        send(es[k].at[here], rd[k].at[here], rd_s.at[k], rd_r.at[k, slot], down)

    def take_up(k, line, count, slot):
        arrived(ru[k].at[pl.ds(line * cb, count * cb)], ru_r.at[k, slot])

    def take_down(k, line, count, slot):
        arrived(rd[k].at[pl.ds(line * cb, count * cb)], rd_r.at[k, slot])

    def add_up(k, line, count):
        def add(at):
            es[k][at, :] += ru[k][at, :]

        in_blocks(line * cb, count * cb, add)

    def add_down(k, line, count):
        def add(at):
            es[k][at, :] += rd[k][at, :]

        in_blocks(line * cb, count * cb, add)

    def rising(k, at):
        if halved(k) or whole(k):
            start = middle if halved(k) else at
            take_up(k, start, lines - start, 0)
            above = max(at + 1, start)
            add_up(k, above, lines - above)
            pass_up(k, above, lines - above, 0)
        else:
            for line in range(last, at, -1):
                take_up(k, line, 1, line)
                add_up(k, line, 1)
                pass_up(k, line, 1, line)

    def falling(k, at):
        if halved(k) or whole(k):
            end = middle if halved(k) else at + 1
            take_down(k, 0, end, 0)
            below = min(at, end)
            add_down(k, 0, below)
            pass_down(k, 0, below, 0)
        else:
            for line in range(at):
                take_down(k, line, 1, line)
                add_down(k, line, 1)
                pass_down(k, line, 1, line)

    def add_near(k):
        for at in range(1, last):

            @pl.when(z == at)
            def _():
                (rising if low(at) else falling)(k, at)

    def add_far(k):
        for at in range(1, last):

            @pl.when(z == at)
            def _():
                (falling if low(at) else rising)(k, at)

    def finish_expr(k):
        for at in range(lines):

            @pl.when(z == at)
            def _():
                if at > 0:
                    if halved(k) and at < middle:
                        take_up(k, at, 1, 1)
                    elif at == last and (halved(k) or whole(k)):
                        take_up(k, at, 1, 0)
                    elif not halved(k) and not whole(k):
                        take_up(k, at, 1, at)
                if at < last:
                    if halved(k) and at >= middle:
                        take_down(k, at, 1, 1)
                    elif at == 0 and (halved(k) or whole(k)):
                        take_down(k, at, 1, 0)
                    elif not halved(k) and not whole(k):
                        take_down(k, at, 1, at)

        from_low, from_high = z > 0, z < last

        @pl.loop(0, cb // BLOCK)
        def _(step):
            here = pl.ds(pl.multiple_of(step * BLOCK, BLOCK), BLOCK)
            own = pl.ds(pl.multiple_of(z * cb + step * BLOCK, BLOCK), BLOCK)
            total = es[k][own, :]
            total = total + jnp.where(from_low, ru[k][own, :], 0.0)
            ge[here, turn_cols(k)] = total + jnp.where(from_high, rd[k][own, :], 0.0)

    def probs_gradient(k):
        at = three_turn_cols(k)

        @pl.loop(0, PLANE * rows // TALL)
        def _(step):
            tall = pl.ds(pl.multiple_of(step * TALL, TALL), TALL)
            part = product(grad_3[tall, at], expr_3[:, at], ((1,), (1,)))
            if k == 0:
                fs[tall, :] = part
            else:
                fs[tall, :] += part

    def slide_of(p, m):
        return pl.ds(pl.multiple_of(p * rows + m * slide_rows, slide_rows), slide_rows)

    def sum_probs_cores():
        for p in mates + (q,):
            fx[p] = fs[slide_of(p, 1 - core), :]
            send(fx.at[p], fy.at[p], fx_s, fx_r.at[p], sibling)

    def return_probs():
        for p in mates:
            arrived(fy.at[p], fx_r.at[p])
            fz[p] = fs[slide_of(p, core), :] + fy[p]
            send(fz.at[p], fr.at[q], f_s, f_r.at[q], mate(p))
        arrived(fy.at[q], fx_r.at[q])
        fr[q] = fs[slide_of(q, core), :] + fy[q]

    def pass_terms():
        for p in mates:
            arrived(l1.at[p], l1_r.at[p])
        l2[z] = (l1[0] + l1[1]) + (l1[2] + l1[3])
        for o in others:
            send(l2.at[z], l2.at[z], l2_s, l2_r.at[z], (o * PLANE + q, core))

    def part_of(slide, m):
        start = slide * slide_rows + m * (slide_rows // 2)
        return pl.ds(pl.multiple_of(start, slide_rows // 2), slide_rows // 2)

    def finish_logits():
        arrived(inn.at[1 - core], in_r)
        rowv[2] = (inn[0] + inn[1]) + rowv[1] * rowv[0]
        for p in mates:
            arrived(fr.at[p], f_r.at[p])
        for m in range(2):

            @pl.loop(0, slide_rows // STEP_ROWS // 2)
            def _(step):
                row_at = (m * (slide_rows // STEP_ROWS // 2) + step) * STEP_ROWS
                at = pl.ds(pl.multiple_of(row_at, STEP_ROWS), STEP_ROWS)
                whole_at = pl.ds(pl.multiple_of(core * slide_rows + row_at, STEP_ROWS), STEP_ROWS)
                by_mass, total_inner = rowv[1, whole_at, 0:1], rowv[2, whole_at, 0:1]
                for p in range(PLANE):
                    for line in range(lines):
                        here, there = pl.ds(line * cb, cb), (line * PLANE + p) * cb
                        grad = fr[p, at, here] + by_mass * weights[:, there : there + cb]
                        glog[whole_at, pl.ds(there, cb)] = pq[p, whole_at, here] * (grad - total_inner)

            here = part_of(core, m)
            send(glog.at[here], glog.at[here], go_s, go_r.at[m], sibling)

    def forward_left():
        for k in range(chunks):

            @pl.when(z < last)
            def _():
                sent(bb[k].at[block(z)], ou_s.at[k])

            @pl.when(z > 0)
            def _():
                sent(bb[k].at[block(z)], od_s.at[k])

            for at in range(1, last):

                @pl.when(z == at)
                def _():
                    sent(bb[k].at[pl.ds(0, at * cb)], fu_s.at[k])
                    sent(bb[k].at[pl.ds((at + 1) * cb, (last - at) * cb)], fd_s.at[k])

        three = pl.ds(0, len(mates))
        sent(ab.at[three, half(0)], a_s)
        sent(ab.at[three, half(0)], a2_s)
        sent(rs.at[three], r_s)
        sent(t0.at[three], t0_s)
        sent(p0.at[three], p0_s)
        for k in range(chunks):
            sent(cr[k].at[three], c_s.at[k])
        sent(s1.at[three], s1_s)
        sent(s2.at[pl.ds(0, last)], s2_s)
        sent(ss.at[0], ss_s)

    steps = {
        "far": forward_far,
        "near": forward_near,
        "next": forward_next,
        "share": share_logits,
        "take": take_probs,
        "whole": gathered,
        "product": forward_product,
        "sum": finish_pred,
        "turn": transpose,
        "plane": sum_plane,
        "line": sum_line,
        "genes": finish_genes,
        "cores": sum_cores,
        "spots": finish_spots,
        "grad": send_grad,
        "terms": send_terms,
        "backward": backward_product,
        "probs": probs_gradient,
        "exchange": sum_probs_cores,
        "return": return_probs,
        "loss": pass_terms,
        "logits": finish_logits,
        "add_near": add_near,
        "add_far": add_far,
        "expr": finish_expr,
        "left": forward_left,
    }
    for name, *where in STEPS:
        steps[name](*where)

    for o in others:
        arrived(l2.at[o], l2_r.at[o])
    loss = l2[0]
    for line in range(1, lines):
        loss = loss + l2[line]
    loss_ref[...] = loss[0:1, 0:1] - (inn[0, 0:1, 1:2] + inn[1, 0:1, 1:2])
    for m in range(2):
        arrived(glog.at[part_of(1 - core, m)], go_r.at[m])

    for k in range(turns):
        for at in range(lines):

            @pl.when(z == at)
            def _():
                if at < last:
                    sent(es[k].at[pl.ds((at + 1) * cb, (last - at) * cb)], ru_s.at[k])
                if at > 0:
                    sent(es[k].at[pl.ds(0, at * cb)], rd_s.at[k])

    three = pl.ds(0, len(mates))
    for k in range(1, turns):
        sent(ds[k].at[pl.ds(0, len(mates) * rows)], d_s.at[k])
    sent(vr.at[three], vr_s)
    sent(inn.at[0], in_s)
    sent(l1.at[three], l1_s)
    sent(l2.at[pl.ds(0, last)], l2_s)
    sent(fr.at[three], f_s)
    sent(fx, fx_s)
    sent(glog.at[half(0)], go_s)


def lane_groups(value):
    parts = [value[:, at : at + LANES] for at in range(0, value.shape[1], LANES)]
    return functools.reduce(lambda a, b: a + b, parts)


def grouped(refs, sizes):
    at = 0
    for size in sizes:
        yield refs[at : at + size]
        at += size


def deliver(pred_in, loss_in, glog_in, gexp_in, pred_ref, loss_ref, glog_ref, gexp_ref, sems):
    slides, slide_rows = pred_ref.shape[0], pred_ref.shape[1]
    pairs = [(gexp_in, gexp_ref), (loss_in, loss_ref)]
    for m in range(slides):
        part = pl.ds(m * slide_rows, slide_rows)
        pairs += [(glog_in.at[part], glog_ref.at[m]), (pred_in.at[part], pred_ref.at[m])]
    copies = [pltpu.make_async_copy(src, dst, sems.at[at]) for at, (src, dst) in enumerate(pairs)]
    for copy in copies:
        copy.start()
    for copy in copies:
        copy.wait()


def plane_call(logits, expr, spatial, slide_spots, spot_cells, cell_prior, lines):
    slides, slide_rows, cells = logits.shape
    rows = slides * slide_rows
    cb, genes = expr.shape
    quarter = lines * cb
    spots = PLANE * rows
    chunks, turns = len(FORWARD), len(BACKWARD)
    dma = pltpu.SemaphoreType.DMA
    vmem = pltpu.VMEM
    anywhere = pl.BlockSpec(memory_space=pl.ANY)
    in_vmem = pl.BlockSpec(memory_space=pltpu.VMEM)
    scratch = [
        pltpu.SMEM((slides,), jnp.int32),
        vmem((slides, slide_rows), jnp.int32),
        vmem((1, cells), jnp.int32),
        vmem((rows, cells), F32),
        vmem((PLANE, slide_rows, quarter), F32),
        vmem((rows, genes), F32),
        vmem((cb, genes), F32),
        vmem((PLANE, rows, quarter), F32),
        vmem((PLANE, rows, quarter), F32),
        vmem((PLANE, rows, quarter), F32),
        vmem((spots, 3 * quarter), BF16),
        vmem((quarter, 3 * spots), BF16),
        vmem((quarter, 3 * genes), BF16),
        vmem((3, rows, LANES), F32),
        vmem((PLANE, 8, genes), F32),
        vmem((lines, 8, genes), F32),
        vmem((8, genes), F32),
        vmem((2, 8, rows), F32),
        vmem((3, rows, LANES), F32),
        vmem((PLANE, 8, rows), F32),
        vmem((spots, 3 * genes), BF16),
        vmem((3 * max(quarter, spots), max(FORWARD + BACKWARD)), BF16),
        vmem((PLANE, rows, BACKWARD[0]), F32),
        vmem((PLANE, rows, BACKWARD[0]), F32),
        vmem((PLANE, 8, rows), F32),
        vmem((spots, quarter), F32),
        vmem((PLANE, slide_rows, quarter), F32),
        vmem((PLANE, slide_rows, quarter), F32),
        vmem((PLANE, slide_rows, quarter), F32),
        vmem((PLANE, slide_rows, quarter), F32),
        vmem((2, rows, LANES), F32),
        vmem((PLANE, 8, LANES), F32),
        vmem((lines, 8, LANES), F32),
        dma((2 * slides + 4,)),
        dma((chunks,)),
        dma((chunks,)),
        dma((chunks,)),
        dma((chunks,)),
        dma((chunks,)),
        dma((chunks, lines)),
        dma((chunks,)),
        dma((chunks, lines)),
        dma,
        dma((PLANE,)),
        dma,
        dma((PLANE,)),
        dma,
        dma((PLANE,)),
        dma((chunks,)),
        dma((chunks, PLANE)),
        dma,
        dma((2, PLANE)),
        dma,
        dma((2, lines)),
        dma,
        dma,
        dma((turns,)),
        dma((turns, PLANE)),
        dma((turns,)),
        dma((turns, lines)),
        dma((turns,)),
        dma((turns, lines)),
        dma,
        dma((PLANE,)),
        dma,
        dma((PLANE,)),
        dma,
        dma((2,)),
        dma,
        dma,
        dma,
        dma((PLANE,)),
        dma,
        dma((lines,)),
        dma,
        dma((PLANE,)),
        dma,
        dma((PLANE,)),
        dma,
        dma((PLANE,)),
    ]
    for shape, widths in (
        ((quarter,), FORWARD),
        ((spots,), FORWARD),
        ((PLANE, rows), FORWARD),
        ((spots,), BACKWARD),
        ((quarter,), BACKWARD),
        ((quarter,), BACKWARD),
        ((quarter,), BACKWARD),
    ):
        scratch += [vmem(shape + (width,), F32) for width in widths]
    in_hbm = functools.partial(pltpu.with_memory_space_constraint, memory_space=pltpu.HBM)
    in_place = functools.partial(pltpu.with_memory_space_constraint, memory_space=pltpu.VMEM)
    results = pl.pallas_call(
        functools.partial(plane_kernel, lines, FORWARD, BACKWARD),
        out_shape=(
            vmem((rows, genes), F32),
            vmem((1, 1), F32),
            vmem((rows, cells), F32),
            vmem((cb, genes), F32),
        ),
        in_specs=[anywhere] * 6,
        out_specs=(in_vmem,) * 4,
        scratch_shapes=scratch,
        compiler_params=pltpu.CompilerParams(
            collective_id=0, has_side_effects=True, vmem_limit_bytes=48 * 1024 * 1024
        ),
    )(*map(in_hbm, (logits, expr, spatial, slide_spots, spot_cells, cell_prior.reshape(1, cells))))
    pred, loss, grad_logits, grad_expr = pl.pallas_call(
        deliver,
        out_shape=(
            jax.ShapeDtypeStruct((slides, slide_rows, genes), F32),
            jax.ShapeDtypeStruct((1, 1), F32),
            jax.ShapeDtypeStruct((slides, slide_rows, cells), F32),
            jax.ShapeDtypeStruct((cb, genes), F32),
        ),
        in_specs=[anywhere] * 4,
        out_specs=(anywhere,) * 4,
        scratch_shapes=[dma((2 * slides + 2,))],
        compiler_params=pltpu.CompilerParams(vmem_limit_bytes=4 * 1024 * 1024),
    )(*map(in_place, results))
    return pred, loss.reshape(()), grad_logits, grad_expr


def general_plan(logits, expr, spatial, slide_spots, spot_cells, cell_prior):
    place = lax.axis_index("spot")
    side = lax.axis_index("gene")
    rows_all = logits.shape[1]
    cell_rows = expr.shape[0]
    weights = cell_prior.astype(jnp.float32) / fixed_point
    gene_share = (place == 0).astype(jnp.float32)
    row_share = (side == 0).astype(jnp.float32)
    own_weights = lax.dynamic_slice_in_dim(weights, place * cell_rows, cell_rows, 0)
    expr_acc = jnp.zeros((cell_rows, expr.shape[1]), jnp.float32)
    loss_local = jnp.zeros((), jnp.float32)
    pred_list = []
    grad_list = []
    for slide in range(logits.shape[0]):
        logit_rows = logits[slide]
        counted = spot_cells[slide].astype(jnp.float32)
        target = spatial[slide]
        positions = place * rows_all + jnp.arange(rows_all, dtype=jnp.int32)
        valid = (positions < slide_spots[slide]).astype(jnp.float32)
        peak = jnp.max(logit_rows, axis=1, keepdims=True)
        raised = jnp.exp(logit_rows - peak)
        probs = raised / jnp.sum(raised, axis=1, keepdims=True)
        mass = jnp.dot(probs, weights, precision=lax.Precision.HIGHEST)
        blocks = lax.all_to_all(probs, "spot", split_axis=1, concat_axis=0, tiled=True)
        pred = lax.psum_scatter(
            jnp.dot(blocks, expr, precision=lax.Precision.HIGHEST),
            "spot",
            scatter_dimension=0,
            tiled=True,
        )
        gene_dot = jnp.sum(valid[:, None] * pred * target, axis=0)
        gene_pred = jnp.sum(valid[:, None] * pred * pred, axis=0)
        gene_true = jnp.sum(valid[:, None] * target * target, axis=0)
        mass_part = jnp.sum(valid * mass)
        kcell = valid * counted
        cell_part = jnp.sum(kcell)
        spot_dot = jnp.sum(pred * target, axis=1)
        spot_pred = jnp.sum(pred * pred, axis=1)
        spot_true = jnp.sum(target * target, axis=1)
        gene_dot, gene_pred, gene_true, mass_total, cell_total = lax.psum(
            (gene_dot, gene_pred, gene_true, mass_part, cell_part), "spot"
        )
        spot_dot, spot_pred, spot_true = lax.psum((spot_dot, spot_pred, spot_true), "gene")
        gene_inv = lax.rsqrt(gene_pred * gene_true + tiny)
        cos_gene = gene_dot * gene_inv
        spot_inv = lax.rsqrt(spot_pred * spot_true + tiny)
        cos_spot = spot_dot * spot_inv
        share = kcell / cell_total
        scale_count = slide_spots[slide].astype(jnp.float32)
        kl_part = jnp.sum(
            share * (jnp.log(counted) - jnp.log(cell_total) - jnp.log(mass) + jnp.log(mass_total))
        )
        loss_local = loss_local - gene_share * jnp.sum(cos_gene)
        loss_local = loss_local + row_share * (scale_count * kl_part - jnp.sum(valid * cos_spot))
        gene_back = cos_gene * gene_true / (gene_pred * gene_true + tiny)
        spot_back = cos_spot * spot_true / (spot_pred * spot_true + tiny)
        dpred = -valid[:, None] * (
            target * (gene_inv[None, :] + spot_inv[:, None])
            - pred * gene_back[None, :]
            - pred * spot_back[:, None]
        )
        dmass = scale_count * valid * (1.0 / mass_total - share / mass)
        pred_list.append(pred)
        grads_full, mass_full = (
            lax.all_gather(dpred, "spot", axis=0, tiled=True),
            lax.all_gather(dmass, "spot", axis=0, tiled=True),
        )
        dprob_cells = jnp.dot(grads_full, expr.T, precision=lax.Precision.HIGHEST)
        dprob_cells = lax.psum(dprob_cells, "gene")
        expr_acc = expr_acc + lax.dot_general(
            blocks, grads_full, (((0,), (0,)), ((), ())), precision=lax.Precision.HIGHEST
        )
        dprob_cells = dprob_cells + mass_full[:, None] * own_weights[None, :]
        dprob_rows = lax.all_to_all(dprob_cells, "spot", split_axis=0, concat_axis=1, tiled=True)
        inner = jnp.sum(probs * dprob_rows, axis=1, keepdims=True)
        dlogit = probs * (dprob_rows - inner)
        grad_list.append(dlogit)
    loss = lax.psum(loss_local, ("spot", "gene"))
    return (jnp.stack(pred_list), loss, jnp.stack(grad_list), expr_acc)


def solution(mesh):
    places = mesh.shape["spot"]

    def on_device(logits, expr, spatial, slide_spots, spot_cells, cell_prior):
        if places == PLANE * PLANE and mesh.shape["gene"] == 2 and expr.shape[1] == sum(FORWARD):
            return plane_call(
                logits, expr, spatial, slide_spots, spot_cells, cell_prior, places // PLANE
            )
        return general_plan(logits, expr, spatial, slide_spots, spot_cells, cell_prior)

    in_specs = (
        P(None, "spot", None),
        P("spot", "gene"),
        P(None, "spot", "gene"),
        P(),
        P(None, "spot"),
        P(),
    )
    out_specs = (P(None, "spot", "gene"), P(), P(None, "spot", None), P("spot", "gene"))
    return jax.shard_map(
        on_device, mesh=mesh, in_specs=in_specs, out_specs=out_specs, check_vma=False
    )
```

```python
import functools

import jax
import jax.numpy as jnp
from jax import lax
from jax.experimental import pallas as pl
from jax.experimental.pallas import tpu as pltpu
from jax.sharding import PartitionSpec as P

tiny = 1e-06
fixed_point = 16384.0
F32 = jnp.float32
BF16 = jnp.bfloat16
MESH = pl.DeviceIdType.MESH

PLANE = 4
LANES = 128
STEP_ROWS = 16
BLOCK = 32
TALL = 256
FORWARD = (128, 256, 256, 128, 128, 128)
BACKWARD = (128, 128, 256, 256, 256)
SPLIT = 4
LEAD = 1
NEAR_LEAD = 2
EARLY = 3
STEPS = (
    ("far", 0),
    ("far", 1),
    ("near", 0),
    ("share",),
    ("far", 2),
    ("far", 3),
    ("take",),
    ("whole", 0),
    ("near", 1),
    ("product", 0),
    ("sum", 0),
    ("whole", 1),
    ("near", 2),
    ("product", 1),
    ("whole", 2),
    ("product", 2),
    ("whole", 3),
    ("near", 3),
    ("product", 3),
    ("far", 4),
    ("whole", 4),
    ("near", 4),
    ("product", 4),
    ("sum", 1),
    ("turn", 0),
    ("far", 5),
    ("whole", 5),
    ("near", 5),
    ("product", 5),
    ("sum", 2),
    ("plane", 0),
    ("turn", 1),
    ("sum", 3),
    ("line", 0),
    ("sum", 4),
    ("sum", 5),
    ("plane", 1),
    ("cores",),
    ("genes", 0),
    ("spots",),
    ("grad", 0),
    ("grad", 1),
    ("grad", 2),
    ("line", 1),
    ("backward", 0),
    ("backward", 1),
    ("add_near", 0),
    ("genes", 1),
    ("grad", 3),
    ("backward", 2),
    ("probs", 0),
    ("add_far", 0),
    ("probs", 1),
    ("expr", 0),
    ("grad", 4),
    ("add_near", 1),
    ("probs", 2),
    ("terms",),
    ("backward", 3),
    ("probs", 3),
    ("add_near", 2),
    ("backward", 4),
    ("add_far", 1),
    ("probs", 4),
    ("exchange",),
    ("add_near", 3),
    ("add_far", 2),
    ("left",),
    ("return",),
    ("loss",),
    ("add_far", 3),
    ("expr", 1),
    ("add_near", 4),
    ("logits",),
    ("add_far", 4),
    ("expr", 2),
    ("expr", 3),
    ("expr", 4),
)


def halves(value):
    high = value.astype(BF16)
    return high, (value - high.astype(F32)).astype(BF16)


def threefold(value):
    high, low = halves(value)
    return jnp.concatenate([high, high, low], axis=1)


def product(a, b, contract):
    return lax.dot_general(a, b, (contract, ((), ())), preferred_element_type=F32)


def plane_kernel(lines, forward_widths, backward_widths, *refs):
    chunks, turns = len(forward_widths), len(backward_widths)
    (
        (logits_ref, expr_ref, spatial_ref, count_in, cells_in, prior_in),
        (pr, loss_ref, glog, ge),
        (count_ref, cells_ref, prior_ref, lg, lq, tg, ex, pq, ab, af, probs_3, turned_3, expr_3, sacc, s1, s2, gv, ss, rowv, rs),
        (grad_3, factor, t0, p0, vr, fs, fx, fy, fz, fr, inn, l1, l2),
        (loc, ou_s, ou_r, od_s, od_r, fu_s, fu_r, fd_s, fd_r, a_s, a_r, a2_s, a2_r, r_s, r_r),
        (c_s, c_r, s1_s, s1_r, s2_s, s2_r, ss_s, ss_r, d_s, d_r, ru_s, ru_r, rd_s, rd_r),
        (f_s, f_r, fx_s, fx_r, go_s, go_r, in_s, in_r, l1_s, l1_r, l2_s, l2_r, t0_s, t0_r, p0_s, p0_r, vr_s, vr_r),
        bb,
        cs,
        cr,
        ds,
        es,
        ru,
        rd,
    ) = grouped(refs, (6, 4, 20, 13, 15, 14, 18, chunks, chunks, chunks, turns, turns, turns, turns))
    place = lax.axis_index("spot")
    core = lax.axis_index("gene")
    z = place // PLANE
    q = place % PLANE
    col, row = q % 2, q // 2
    mates = ((1 - row) * 2 + 1 - col, row * 2 + 1 - col, (1 - row) * 2 + col)
    others = tuple((z + step) % lines for step in range(1, lines))
    up, down = (place + PLANE, core), (place - PLANE, core)
    sibling = (place, 1 - core)
    slides, slide_rows = logits_ref.shape[0], logits_ref.shape[1]
    rows = slides * slide_rows
    cb = expr_ref.shape[0]
    genes = expr_ref.shape[1]
    last = lines - 1

    def mate(p):
        return (z * PLANE + p, core)

    def send(src, dst, send_sem, recv_sem, device):
        copy = pltpu.make_async_remote_copy(
            src_ref=src, dst_ref=dst, send_sem=send_sem, recv_sem=recv_sem, device_id=device, device_id_type=MESH
        )
        copy.start()

    def arrived(dst, recv_sem):
        pltpu.make_async_copy(dst, dst, recv_sem).wait()

    sent = arrived

    def cols(k):
        return pl.ds(sum(forward_widths[:k]), forward_widths[k])

    def turn_cols(k):
        return pl.ds(sum(backward_widths[:k]), backward_widths[k])

    def block(index):
        return pl.ds(pl.multiple_of(index * cb, cb), cb)

    def share(index):
        return pl.ds(pl.multiple_of(index * rows, rows), rows)

    def half(index):
        return pl.ds(pl.multiple_of(index * slide_rows, slide_rows), slide_rows)

    small = ((prior_in, prior_ref), (count_in, count_ref), (cells_in, cells_ref))
    pltpu.make_async_copy(expr_ref, ex, loc.at[2 * slides]).start()
    for m in range(slides):
        pltpu.make_async_copy(logits_ref.at[m], lg.at[half(m)], loc.at[m]).start()
    for at, (src, dst) in enumerate(small):
        pltpu.make_async_copy(src, dst, loc.at[2 * slides + 1 + at]).start()
    for m in range(slides):
        pltpu.make_async_copy(spatial_ref.at[m], tg.at[half(m)], loc.at[slides + m]).start()

    barrier = pltpu.get_barrier_semaphore()
    for p in mates:
        pl.semaphore_signal(barrier, inc=1, device_id=mate(p), device_id_type=MESH)
    for o in others:
        pl.semaphore_signal(barrier, inc=1, device_id=(o * PLANE + q, core), device_id_type=MESH)
    pl.semaphore_signal(barrier, inc=1, device_id=sibling, device_id_type=MESH)
    pltpu.make_async_copy(expr_ref, ex, loc.at[2 * slides]).wait()
    for k in range(chunks):
        bb[k][block(z), :] = ex[:, cols(k)]
    for m in range(slides):
        pltpu.make_async_copy(logits_ref.at[m], lg.at[half(m)], loc.at[m]).wait()
    for p in range(PLANE):
        for line in range(lines):
            lq[p, :, pl.ds(line * cb, cb)] = lg[half(core), pl.ds((line * PLANE + p) * cb, cb)]
    pl.semaphore_wait(barrier, len(mates) + len(others) + 1)

    def own_up(k):
        here = bb[k].at[block(z)]
        send(here, here, ou_s.at[k], ou_r.at[k], up)

    def own_down(k):
        here = bb[k].at[block(z)]
        send(here, here, od_s.at[k], od_r.at[k], down)

    def low(at):
        return 2 * at < lines

    for at in range(lines):

        @pl.when(z == at)
        def _():
            for k in range(chunks):
                if at < last and (at == 0 or k < (LEAD if low(at) else NEAR_LEAD)):
                    own_up(k)
                if at > 0 and (at == last or k < (NEAR_LEAD if low(at) else LEAD)):
                    own_down(k)

    for p in mates:
        send(lq.at[p], ab.at[q, half(core)], a_s, a_r.at[q], mate(p))

    def from_below(k, at):
        arrived(bb[k].at[pl.ds((at - 1) * cb, cb)], ou_r.at[k])
        if at > 1:
            arrived(bb[k].at[pl.ds(0, (at - 1) * cb)], fu_r.at[k])

    def from_above(k, at):
        arrived(bb[k].at[pl.ds((at + 1) * cb, cb)], od_r.at[k])
        if at < last - 1:
            arrived(bb[k].at[pl.ds((at + 2) * cb, (last - 1 - at) * cb)], fd_r.at[k])

    def upward(k, at):
        from_below(k, at)
        here = bb[k].at[pl.ds(0, at * cb)]
        send(here, here, fu_s.at[k], fu_r.at[k], up)

    def downward(k, at):
        from_above(k, at)
        here = bb[k].at[pl.ds((at + 1) * cb, (last - at) * cb)]
        send(here, here, fd_s.at[k], fd_r.at[k], down)

    def forward_far(k):
        for at in range(1, last):

            @pl.when(z == at)
            def _():
                (upward if low(at) else downward)(k, at)
                if k + LEAD < chunks:
                    (own_up if low(at) else own_down)(k + LEAD)

    def forward_near(k):
        for at in range(1, last):

            @pl.when(z == at)
            def _():
                (downward if low(at) else upward)(k, at)
                if k + NEAR_LEAD < chunks:
                    (own_down if low(at) else own_up)(k + NEAR_LEAD)

    def gathered(k):
        @pl.when(z == 0)
        def _():
            from_above(k, 0)

        @pl.when(z == last)
        def _():
            from_below(k, last)

    for at, (src, dst) in enumerate(small):
        pltpu.make_async_copy(src, dst, loc.at[2 * slides + 1 + at]).wait()
    weights = prior_ref[...].astype(F32) / fixed_point

    @pl.loop(0, rows // STEP_ROWS)
    def _(step):
        at = pl.ds(pl.multiple_of(step * STEP_ROWS, STEP_ROWS), STEP_ROWS)
        value = lg[at, :]
        peak = jnp.max(value, axis=1, keepdims=True)
        raised = jnp.exp(value - peak)
        scale = 1.0 / jnp.sum(raised, axis=1, keepdims=True)
        probs = raised * scale
        mass_rows = jnp.sum(probs * weights, axis=1, keepdims=True)
        rowv[0, at, :] = jnp.broadcast_to(mass_rows, (STEP_ROWS, LANES))
        rowv[1, at, :] = jnp.broadcast_to(peak, (STEP_ROWS, LANES))
        rowv[2, at, :] = jnp.broadcast_to(scale, (STEP_ROWS, LANES))
        for p in range(PLANE):
            for line in range(lines):
                at_cells = (line * PLANE + p) * cb
                pq[p, at, pl.ds(line * cb, cb)] = probs[:, at_cells : at_cells + cb]

    wide = lax.broadcasted_iota(jnp.int32, (rows, LANES), 1)
    rs[q] = jnp.where(wide == 0, rowv[1], rowv[2]).T[0:8]
    for p in mates:
        send(rs.at[q], rs.at[q], r_s, r_r.at[q], mate(p))

    rid = lax.broadcasted_iota(jnp.int32, (rows, 1), 0)
    first = rid < slide_rows
    position = place * slide_rows + jnp.where(first, rid, rid - slide_rows)
    count = jnp.where(first, count_ref[0], count_ref[1])
    valid = (position < count).astype(F32)
    scale_count = count.astype(F32)
    square = (slide_rows, slide_rows)
    eye = lax.broadcasted_iota(jnp.int32, square, 0) == lax.broadcasted_iota(jnp.int32, square, 1)
    counted = jnp.concatenate(
        [
            jnp.sum(jnp.where(eye, cells_ref[m : m + 1, :].astype(F32), 0.0), axis=1, keepdims=True)
            for m in range(slides)
        ],
        axis=0,
    )
    mass = rowv[0, :, 0:1]
    kcell = valid * counted

    def by_slide(value):
        return [jnp.sum(value[m * slide_rows : (m + 1) * slide_rows], axis=0, keepdims=True) for m in range(slides)]

    mass_parts = by_slide(valid * mass)
    cell_parts = by_slide(kcell)
    lane = lax.broadcasted_iota(jnp.int32, (1, LANES), 1)
    scalars = jnp.zeros((1, LANES), F32)
    for at, value in enumerate(mass_parts + cell_parts):
        scalars = jnp.where(lane == at, value, scalars)
    for m in range(slides):
        pltpu.make_async_copy(spatial_ref.at[m], tg.at[half(m)], loc.at[slides + m]).wait()

    head = backward_widths[0]
    t0[q] = tg[:, 0:head]
    for p in mates:
        send(t0.at[q], t0.at[q], t0_s, t0_r.at[q], mate(p))
    sacc[...] = jnp.zeros_like(sacc)
    s1[q, 3 * slides :, :] = jnp.zeros((8 - 3 * slides, genes), F32)
    s1[q, 3 * slides : 3 * slides + 1, 0:LANES] = scalars

    def share_logits():
        for p in (mates[1], mates[2], mates[0]):
            here = ab.at[p, half(core)]
            arrived(here, a_r.at[p])
            send(here, here, a2_s, a2_r.at[p], sibling)

    def lay_probs(p, at, value):
        af[p, at, :] = value
        there = pl.ds(pl.multiple_of(p * rows + at.start, BLOCK), BLOCK)
        probs_3[there, :] = threefold(value)

    def take_probs():
        in_blocks(0, rows, lambda at: lay_probs(q, at, pq[q, at, :]))
        for p in (mates[1], mates[2], mates[0]):
            arrived(rs.at[p], r_r.at[p])
            arrived(ab.at[p, half(1 - core)], a2_r.at[p])
            rowv[1] = jnp.concatenate([rs[p].T, jnp.zeros((rows, LANES - 8), F32)], axis=1)

            def take(at):
                probs = jnp.exp(ab[p, at, :] - rowv[1, at, 0:1]) * rowv[1, at, 1:2]
                lay_probs(p, at, probs)

            in_blocks(0, rows, take)

    def transpose(part):
        @pl.loop(0, PLANE // 2)
        def _(step):
            p = part * (PLANE // 2) + step
            high, low_part = halves(af[p].T)
            for third, value in enumerate((high, high, low_part)):
                turned_3[:, pl.ds(pl.multiple_of(third * PLANE * rows + p * rows, rows), rows)] = value

    def in_blocks(start, count, body):
        @pl.loop(0, count // BLOCK)
        def _(step):
            body(pl.ds(pl.multiple_of(start + step * BLOCK, BLOCK), BLOCK))

    quarter = lines * cb

    def lay_factor(at, length, width, value):
        high, low_part = halves(value)
        for third, part in enumerate((high, low_part, high)):
            here = pl.ds(pl.multiple_of(third * length + at.start, BLOCK), BLOCK)
            factor[here, 0:width] = part

    def keep_expr(k, at, value):
        start = sum(forward_widths[:k])
        for turn in range(turns):
            origin, width = sum(backward_widths[:turn]), backward_widths[turn]
            lo, hi = max(start, origin), min(start + forward_widths[k], origin + width)
            if lo < hi:
                high, low_part = halves(value[:, lo - start : hi - start])
                for third, part in enumerate((high, low_part, high)):
                    expr_3[at, pl.ds(3 * origin + third * width + lo - origin, hi - lo)] = part

    def three_turn_cols(k):
        return pl.ds(3 * sum(backward_widths[:k]), 3 * backward_widths[k])

    def forward_product(k):
        width = forward_widths[k]

        def lay(at):
            value = bb[k][at, :]
            lay_factor(at, quarter, width, value)
            keep_expr(k, at, value)

        in_blocks(0, quarter, lay)
        if k < chunks - 1:

            @pl.loop(0, PLANE * rows // TALL)
            def _(step):
                tall = pl.ds(pl.multiple_of(step * TALL, TALL), TALL)
                cs[k][tall, :] = product(probs_3[tall, :], factor[0 : 3 * quarter, 0:width], ((1,), (0,)))

            for p in mates:
                pass_pred(k, p)
        else:
            for side, served in ((1 - row, (mates[0], mates[2])), (row, (mates[1],))):
                pair = pl.ds(pl.multiple_of(2 * side * rows, 2 * rows), 2 * rows)
                cs[k][pair, :] = product(probs_3[pair, :], factor[0 : 3 * quarter, 0:width], ((1,), (0,)))
                for p in served:
                    pass_pred(k, p)

    def pass_pred(k, p):
        send(cs[k].at[share(p)], cr[k].at[q], c_s.at[k], c_r.at[k, q], mate(p))

    def finish_pred(k):
        total = cs[k][share(q), :]
        for p in mates:
            arrived(cr[k].at[p], c_r.at[k, p])
            total = total + cr[k][p]
        pr[:, cols(k)] = total
        if k == 0:
            p0[q] = total[:, 0:head]
            for p in mates:
                send(p0.at[q], p0.at[q], p0_s, p0_r.at[q], mate(p))
        truth = tg[:, cols(k)]
        for at, value in enumerate((total * truth, total * total, truth * truth)):
            sacc[at] += lane_groups(value)
        kept = valid * total
        stats = by_slide(kept * truth) + by_slide(kept * total) + by_slide(valid * truth * truth)
        s1[q, 0 : 3 * slides, cols(k)] = jnp.concatenate(stats, axis=0)

    early = sum(forward_widths[:EARLY])
    parts = (pl.ds(0, early), pl.ds(early, genes - early))

    def sum_plane(at):
        for p in mates:
            send(s1.at[q, :, parts[at]], s1.at[q, :, parts[at]], s1_s, s1_r.at[at, q], mate(p))

    def sum_line(at):
        for p in mates:
            arrived(s1.at[p, :, parts[at]], s1_r.at[at, p])
        s2[z, :, parts[at]] = (s1[0, :, parts[at]] + s1[1, :, parts[at]]) + (s1[2, :, parts[at]] + s1[3, :, parts[at]])
        for o in others:
            send(s2.at[z, :, parts[at]], s2.at[z, :, parts[at]], s2_s, s2_r.at[at, z], (o * PLANE + q, core))

    kept = {}

    def finish_genes(at):
        for o in others:
            arrived(s2.at[o, :, parts[at]], s2_r.at[at, o])
        total = s2[0, :, parts[at]]
        for line in range(1, lines):
            total = total + s2[line, :, parts[at]]
        gene_dot, gene_pred, gene_true = total[0:2], total[2:4], total[4:6]
        gene_inv = lax.rsqrt(gene_pred * gene_true + tiny)
        cos_gene = gene_dot * gene_inv
        gv[0:2, parts[at]] = gene_inv
        gv[2:4, parts[at]] = cos_gene * gene_true / (gene_pred * gene_true + tiny)
        kept["genes", at] = jnp.sum(jnp.sum(cos_gene, axis=1, keepdims=True), axis=0, keepdims=True)
        if at == 0:
            kept["mass"] = jnp.where(first, total[6:7, 0:1], total[6:7, 1:2])
            kept["cells"] = jnp.where(first, total[6:7, 2:3], total[6:7, 3:4])

    def sum_cores():
        sums = [jnp.sum(sacc[at], axis=1, keepdims=True) for at in range(3)]
        ss[core] = jnp.where(wide == 0, sums[0], jnp.where(wide == 1, sums[1], sums[2])).T[0:8]
        send(ss.at[core], ss.at[core], ss_s, ss_r, sibling)

    def finish_spots():
        lane_id = lax.broadcasted_iota(jnp.int32, (1, rows), 1)
        first_lane = lane_id < slide_rows
        lane_position = place * slide_rows + jnp.where(first_lane, lane_id, lane_id - slide_rows)
        lane_valid = (lane_position < jnp.where(first_lane, count_ref[0], count_ref[1])).astype(F32)
        arrived(ss.at[1 - core], ss_r)
        spot = ss[0] + ss[1]
        spot_dot, spot_pred, spot_true = spot[0:1], spot[1:2], spot[2:3]
        spot_inv = lax.rsqrt(spot_pred * spot_true + tiny)
        cos_spot = spot_dot * spot_inv
        spot_back = cos_spot * spot_true / (spot_pred * spot_true + tiny)
        kept["cos"] = jnp.sum(lane_valid * cos_spot, axis=1, keepdims=True)
        vectors = [lane_valid * spot_inv, lane_valid * spot_back, lane_valid, jnp.zeros((5, rows), F32)]
        vr[q] = jnp.concatenate(vectors, axis=0)
        sacc[0] = jnp.zeros_like(sacc[0])

    def gradient(truth, guess, by_row, k):
        pieces = []
        for m in range(slides):
            lo, hi = m * slide_rows, (m + 1) * slide_rows
            inverse, back = gv[m : m + 1, turn_cols(k)], gv[2 + m : 3 + m, turn_cols(k)]
            spot_inv, spot_back, spot_valid = by_row[lo:hi, 0:1], by_row[lo:hi, 1:2], by_row[lo:hi, 2:3]
            pieces.append(
                guess[lo:hi] * (spot_valid * back + spot_back) - truth[lo:hi] * (spot_valid * inverse + spot_inv)
            )
        return jnp.concatenate(pieces, axis=0)

    def head_gradient():
        for p in mates:
            arrived(t0.at[p], t0_r.at[p])
            arrived(p0.at[p], p0_r.at[p])
            arrived(vr.at[p], vr_r.at[p])
        for p in range(PLANE):
            ds[0][share(p), :] = gradient(t0[p], p0[p], vr[p].T, 0)
        sacc[0] += lane_groups(ds[0][share(q), :] * p0[q])

    def send_grad(k):
        if k == 0:
            for p in mates:
                send(vr.at[q], vr.at[q], vr_s, vr_r.at[q], mate(p))
            kept["by_row"] = vr[q].T
            return
        grad = gradient(tg[:, turn_cols(k)], pr[:, turn_cols(k)], kept["by_row"], k)
        here = ds[k].at[share(q)]
        here[...] = grad
        for p in mates:
            send(here, here, d_s.at[k], d_r.at[k, q], mate(p))
        sacc[0] += lane_groups(grad * pr[:, turn_cols(k)])

    def send_terms():
        mass_total, cell_total = kept["mass"], kept["cells"]
        portion = kcell / cell_total
        kl_rows = portion * (jnp.log(counted) - jnp.log(cell_total) - jnp.log(mass) + jnp.log(mass_total))
        dmass = scale_count * valid * (1.0 / mass_total - portion / mass)
        terms = jnp.sum(scale_count * kl_rows, axis=0, keepdims=True) - kept["cos"]
        l1[q] = jnp.broadcast_to(terms, (8, LANES))
        for p in mates:
            send(l1.at[q], l1.at[q], l1_s, l1_r.at[q], mate(p))
        inner = jnp.sum(sacc[0], axis=1, keepdims=True)
        inn[core] = jnp.where(wide == 0, inner, kept["genes", 0] + kept["genes", 1])
        send(inn.at[core], inn.at[core], in_s, in_r, sibling)
        rowv[1] = jnp.broadcast_to(dmass, (rows, LANES))

    middle = lines // 2

    def backward_product(k):
        if k == 0:
            head_gradient()
        else:
            for p in mates:
                arrived(ds[k].at[share(p)], d_r.at[k, p])
        width, spots = backward_widths[k], PLANE * rows

        def lay(at):
            value = ds[k][at, :]
            lay_factor(at, spots, width, value)
            grad_3[at, three_turn_cols(k)] = threefold(value)

        in_blocks(0, spots, lay)
        if not halved(k):

            @pl.loop(0, quarter // TALL)
            def _(step):
                tall = pl.ds(pl.multiple_of(step * TALL, TALL), TALL)
                es[k][tall, :] = product(turned_3[tall, :], factor[0 : 3 * spots, 0:width], ((1,), (0,)))

        for turn in range(2):
            if halved(k):
                side = (1 - z // middle) if turn == 0 else z // middle
                pair = pl.ds(pl.multiple_of(side * middle * cb, middle * cb), middle * cb)
                es[k][pair, :] = product(turned_3[pair, :], factor[0 : 3 * spots, 0:width], ((1,), (0,)))

            @pl.when(z == 0)
            def _():
                if halved(k):
                    pass_up(k, middle if turn == 0 else 1, middle if turn == 0 else middle - 1, turn)
                elif whole(k):
                    if turn == 0:
                        pass_up(k, 1, last, 0)
                elif turn == 0:
                    for line in range(last, 0, -1):
                        pass_up(k, line, 1, line)

            @pl.when(z == last)
            def _():
                if halved(k):
                    pass_down(k, 0 if turn == 0 else middle, middle if turn == 0 else middle - 1, turn)
                elif whole(k):
                    if turn == 0:
                        pass_down(k, 0, last, 0)
                elif turn == 0:
                    for line in range(last):
                        pass_down(k, line, 1, line)

    def halved(k):
        return k == 0

    def whole(k):
        return 0 < k < turns - SPLIT

    def pass_up(k, line, count, slot):
        here = pl.ds(line * cb, count * cb)
        send(es[k].at[here], ru[k].at[here], ru_s.at[k], ru_r.at[k, slot], up)

    def pass_down(k, line, count, slot):
        here = pl.ds(line * cb, count * cb)
        send(es[k].at[here], rd[k].at[here], rd_s.at[k], rd_r.at[k, slot], down)

    def take_up(k, line, count, slot):
        arrived(ru[k].at[pl.ds(line * cb, count * cb)], ru_r.at[k, slot])

    def take_down(k, line, count, slot):
        arrived(rd[k].at[pl.ds(line * cb, count * cb)], rd_r.at[k, slot])

    def add_up(k, line, count):
        def add(at):
            es[k][at, :] += ru[k][at, :]

        in_blocks(line * cb, count * cb, add)

    def add_down(k, line, count):
        def add(at):
            es[k][at, :] += rd[k][at, :]

        in_blocks(line * cb, count * cb, add)

    def rising(k, at):
        if halved(k) or whole(k):
            start = middle if halved(k) else at
            take_up(k, start, lines - start, 0)
            above = max(at + 1, start)
            add_up(k, above, lines - above)
            pass_up(k, above, lines - above, 0)
        else:
            for line in range(last, at, -1):
                take_up(k, line, 1, line)
                add_up(k, line, 1)
                pass_up(k, line, 1, line)

    def falling(k, at):
        if halved(k) or whole(k):
            end = middle if halved(k) else at + 1
            take_down(k, 0, end, 0)
            below = min(at, end)
            add_down(k, 0, below)
            pass_down(k, 0, below, 0)
        else:
            for line in range(at):
                take_down(k, line, 1, line)
                add_down(k, line, 1)
                pass_down(k, line, 1, line)

    def add_near(k):
        for at in range(1, last):

            @pl.when(z == at)
            def _():
                (rising if low(at) else falling)(k, at)

    def add_far(k):
        for at in range(1, last):

            @pl.when(z == at)
            def _():
                (falling if low(at) else rising)(k, at)

    def finish_expr(k):
        for at in range(lines):

            @pl.when(z == at)
            def _():
                if at > 0:
                    if halved(k) and at < middle:
                        take_up(k, at, 1, 1)
                    elif at == last and (halved(k) or whole(k)):
                        take_up(k, at, 1, 0)
                    elif not halved(k) and not whole(k):
                        take_up(k, at, 1, at)
                if at < last:
                    if halved(k) and at >= middle:
                        take_down(k, at, 1, 1)
                    elif at == 0 and (halved(k) or whole(k)):
                        take_down(k, at, 1, 0)
                    elif not halved(k) and not whole(k):
                        take_down(k, at, 1, at)

        from_low, from_high = z > 0, z < last

        @pl.loop(0, cb // BLOCK)
        def _(step):
            here = pl.ds(pl.multiple_of(step * BLOCK, BLOCK), BLOCK)
            own = pl.ds(pl.multiple_of(z * cb + step * BLOCK, BLOCK), BLOCK)
            total = es[k][own, :]
            total = total + jnp.where(from_low, ru[k][own, :], 0.0)
            ge[here, turn_cols(k)] = total + jnp.where(from_high, rd[k][own, :], 0.0)

    def probs_gradient(k):
        at = three_turn_cols(k)

        @pl.loop(0, PLANE * rows // TALL)
        def _(step):
            tall = pl.ds(pl.multiple_of(step * TALL, TALL), TALL)
            part = product(grad_3[tall, at], expr_3[:, at], ((1,), (1,)))
            if k == 0:
                fs[tall, :] = part
            else:
                fs[tall, :] += part

    def slide_of(p, m):
        return pl.ds(pl.multiple_of(p * rows + m * slide_rows, slide_rows), slide_rows)

    def sum_probs_cores():
        for p in mates + (q,):
            fx[p] = fs[slide_of(p, 1 - core), :]
            send(fx.at[p], fy.at[p], fx_s, fx_r.at[p], sibling)

    def return_probs():
        for p in mates:
            arrived(fy.at[p], fx_r.at[p])
            fz[p] = fs[slide_of(p, core), :] + fy[p]
            send(fz.at[p], fr.at[q], f_s, f_r.at[q], mate(p))
        arrived(fy.at[q], fx_r.at[q])
        fr[q] = fs[slide_of(q, core), :] + fy[q]

    def pass_terms():
        for p in mates:
            arrived(l1.at[p], l1_r.at[p])
        l2[z] = (l1[0] + l1[1]) + (l1[2] + l1[3])
        for o in others:
            send(l2.at[z], l2.at[z], l2_s, l2_r.at[z], (o * PLANE + q, core))

    def part_of(slide, m):
        start = slide * slide_rows + m * (slide_rows // 2)
        return pl.ds(pl.multiple_of(start, slide_rows // 2), slide_rows // 2)

    def finish_logits():
        arrived(inn.at[1 - core], in_r)
        rowv[2] = (inn[0] + inn[1]) + rowv[1] * rowv[0]
        for p in mates:
            arrived(fr.at[p], f_r.at[p])
        for m in range(2):

            @pl.loop(0, slide_rows // STEP_ROWS // 2)
            def _(step):
                row_at = (m * (slide_rows // STEP_ROWS // 2) + step) * STEP_ROWS
                at = pl.ds(pl.multiple_of(row_at, STEP_ROWS), STEP_ROWS)
                whole_at = pl.ds(pl.multiple_of(core * slide_rows + row_at, STEP_ROWS), STEP_ROWS)
                by_mass, total_inner = rowv[1, whole_at, 0:1], rowv[2, whole_at, 0:1]
                for p in range(PLANE):
                    for line in range(lines):
                        here, there = pl.ds(line * cb, cb), (line * PLANE + p) * cb
                        grad = fr[p, at, here] + by_mass * weights[:, there : there + cb]
                        glog[whole_at, pl.ds(there, cb)] = pq[p, whole_at, here] * (grad - total_inner)

            here = part_of(core, m)
            send(glog.at[here], glog.at[here], go_s, go_r.at[m], sibling)

    def forward_left():
        for k in range(chunks):

            @pl.when(z < last)
            def _():
                sent(bb[k].at[block(z)], ou_s.at[k])

            @pl.when(z > 0)
            def _():
                sent(bb[k].at[block(z)], od_s.at[k])

            for at in range(1, last):

                @pl.when(z == at)
                def _():
                    sent(bb[k].at[pl.ds(0, at * cb)], fu_s.at[k])
                    sent(bb[k].at[pl.ds((at + 1) * cb, (last - at) * cb)], fd_s.at[k])

        three = pl.ds(0, len(mates))
        sent(ab.at[three, half(0)], a_s)
        sent(ab.at[three, half(0)], a2_s)
        sent(rs.at[three], r_s)
        sent(t0.at[three], t0_s)
        sent(p0.at[three], p0_s)
        for k in range(chunks):
            sent(cr[k].at[three], c_s.at[k])
        sent(s1.at[three], s1_s)
        sent(s2.at[pl.ds(0, last)], s2_s)
        sent(ss.at[0], ss_s)

    steps = {
        "far": forward_far,
        "near": forward_near,
        "share": share_logits,
        "take": take_probs,
        "whole": gathered,
        "product": forward_product,
        "sum": finish_pred,
        "turn": transpose,
        "plane": sum_plane,
        "line": sum_line,
        "genes": finish_genes,
        "cores": sum_cores,
        "spots": finish_spots,
        "grad": send_grad,
        "terms": send_terms,
        "backward": backward_product,
        "probs": probs_gradient,
        "exchange": sum_probs_cores,
        "return": return_probs,
        "loss": pass_terms,
        "logits": finish_logits,
        "add_near": add_near,
        "add_far": add_far,
        "expr": finish_expr,
        "left": forward_left,
    }
    for name, *where in STEPS:
        steps[name](*where)

    for o in others:
        arrived(l2.at[o], l2_r.at[o])
    loss = l2[0]
    for line in range(1, lines):
        loss = loss + l2[line]
    loss_ref[...] = loss[0:1, 0:1] - (inn[0, 0:1, 1:2] + inn[1, 0:1, 1:2])
    for m in range(2):
        arrived(glog.at[part_of(1 - core, m)], go_r.at[m])

    for k in range(turns):
        for at in range(lines):

            @pl.when(z == at)
            def _():
                if at < last:
                    sent(es[k].at[pl.ds((at + 1) * cb, (last - at) * cb)], ru_s.at[k])
                if at > 0:
                    sent(es[k].at[pl.ds(0, at * cb)], rd_s.at[k])

    three = pl.ds(0, len(mates))
    for k in range(1, turns):
        sent(ds[k].at[pl.ds(0, len(mates) * rows)], d_s.at[k])
    sent(vr.at[three], vr_s)
    sent(inn.at[0], in_s)
    sent(l1.at[three], l1_s)
    sent(l2.at[pl.ds(0, last)], l2_s)
    sent(fr.at[three], f_s)
    sent(fx, fx_s)
    sent(glog.at[half(0)], go_s)


def lane_groups(value):
    parts = [value[:, at : at + LANES] for at in range(0, value.shape[1], LANES)]
    return functools.reduce(lambda a, b: a + b, parts)


def grouped(refs, sizes):
    at = 0
    for size in sizes:
        yield refs[at : at + size]
        at += size


def deliver(pred_in, loss_in, glog_in, gexp_in, pred_ref, loss_ref, glog_ref, gexp_ref, sems):
    slides, slide_rows = pred_ref.shape[0], pred_ref.shape[1]
    pairs = [(gexp_in, gexp_ref), (loss_in, loss_ref)]
    for m in range(slides):
        part = pl.ds(m * slide_rows, slide_rows)
        pairs += [(glog_in.at[part], glog_ref.at[m]), (pred_in.at[part], pred_ref.at[m])]
    copies = [pltpu.make_async_copy(src, dst, sems.at[at]) for at, (src, dst) in enumerate(pairs)]
    for copy in copies:
        copy.start()
    for copy in copies:
        copy.wait()


def plane_call(logits, expr, spatial, slide_spots, spot_cells, cell_prior, lines):
    slides, slide_rows, cells = logits.shape
    rows = slides * slide_rows
    cb, genes = expr.shape
    quarter = lines * cb
    spots = PLANE * rows
    chunks, turns = len(FORWARD), len(BACKWARD)
    dma = pltpu.SemaphoreType.DMA
    vmem = pltpu.VMEM
    anywhere = pl.BlockSpec(memory_space=pl.ANY)
    in_vmem = pl.BlockSpec(memory_space=pltpu.VMEM)
    scratch = [
        pltpu.SMEM((slides,), jnp.int32),
        vmem((slides, slide_rows), jnp.int32),
        vmem((1, cells), jnp.int32),
        vmem((rows, cells), F32),
        vmem((PLANE, slide_rows, quarter), F32),
        vmem((rows, genes), F32),
        vmem((cb, genes), F32),
        vmem((PLANE, rows, quarter), F32),
        vmem((PLANE, rows, quarter), F32),
        vmem((PLANE, rows, quarter), F32),
        vmem((spots, 3 * quarter), BF16),
        vmem((quarter, 3 * spots), BF16),
        vmem((quarter, 3 * genes), BF16),
        vmem((3, rows, LANES), F32),
        vmem((PLANE, 8, genes), F32),
        vmem((lines, 8, genes), F32),
        vmem((8, genes), F32),
        vmem((2, 8, rows), F32),
        vmem((3, rows, LANES), F32),
        vmem((PLANE, 8, rows), F32),
        vmem((spots, 3 * genes), BF16),
        vmem((3 * max(quarter, spots), max(FORWARD + BACKWARD)), BF16),
        vmem((PLANE, rows, BACKWARD[0]), F32),
        vmem((PLANE, rows, BACKWARD[0]), F32),
        vmem((PLANE, 8, rows), F32),
        vmem((spots, quarter), F32),
        vmem((PLANE, slide_rows, quarter), F32),
        vmem((PLANE, slide_rows, quarter), F32),
        vmem((PLANE, slide_rows, quarter), F32),
        vmem((PLANE, slide_rows, quarter), F32),
        vmem((2, rows, LANES), F32),
        vmem((PLANE, 8, LANES), F32),
        vmem((lines, 8, LANES), F32),
        dma((2 * slides + 4,)),
        dma((chunks,)),
        dma((chunks,)),
        dma((chunks,)),
        dma((chunks,)),
        dma((chunks,)),
        dma((chunks,)),
        dma((chunks,)),
        dma((chunks,)),
        dma,
        dma((PLANE,)),
        dma,
        dma((PLANE,)),
        dma,
        dma((PLANE,)),
        dma((chunks,)),
        dma((chunks, PLANE)),
        dma,
        dma((2, PLANE)),
        dma,
        dma((2, lines)),
        dma,
        dma,
        dma((turns,)),
        dma((turns, PLANE)),
        dma((turns,)),
        dma((turns, lines)),
        dma((turns,)),
        dma((turns, lines)),
        dma,
        dma((PLANE,)),
        dma,
        dma((PLANE,)),
        dma,
        dma((2,)),
        dma,
        dma,
        dma,
        dma((PLANE,)),
        dma,
        dma((lines,)),
        dma,
        dma((PLANE,)),
        dma,
        dma((PLANE,)),
        dma,
        dma((PLANE,)),
    ]
    for shape, widths in (
        ((quarter,), FORWARD),
        ((spots,), FORWARD),
        ((PLANE, rows), FORWARD),
        ((spots,), BACKWARD),
        ((quarter,), BACKWARD),
        ((quarter,), BACKWARD),
        ((quarter,), BACKWARD),
    ):
        scratch += [vmem(shape + (width,), F32) for width in widths]
    in_hbm = functools.partial(pltpu.with_memory_space_constraint, memory_space=pltpu.HBM)
    in_place = functools.partial(pltpu.with_memory_space_constraint, memory_space=pltpu.VMEM)
    results = pl.pallas_call(
        functools.partial(plane_kernel, lines, FORWARD, BACKWARD),
        out_shape=(
            vmem((rows, genes), F32),
            vmem((1, 1), F32),
            vmem((rows, cells), F32),
            vmem((cb, genes), F32),
        ),
        in_specs=[anywhere] * 6,
        out_specs=(in_vmem,) * 4,
        scratch_shapes=scratch,
        compiler_params=pltpu.CompilerParams(
            collective_id=0, has_side_effects=True, vmem_limit_bytes=48 * 1024 * 1024
        ),
    )(*map(in_hbm, (logits, expr, spatial, slide_spots, spot_cells, cell_prior.reshape(1, cells))))
    pred, loss, grad_logits, grad_expr = pl.pallas_call(
        deliver,
        out_shape=(
            jax.ShapeDtypeStruct((slides, slide_rows, genes), F32),
            jax.ShapeDtypeStruct((1, 1), F32),
            jax.ShapeDtypeStruct((slides, slide_rows, cells), F32),
            jax.ShapeDtypeStruct((cb, genes), F32),
        ),
        in_specs=[anywhere] * 4,
        out_specs=(anywhere,) * 4,
        scratch_shapes=[dma((2 * slides + 2,))],
        compiler_params=pltpu.CompilerParams(vmem_limit_bytes=4 * 1024 * 1024),
    )(*map(in_place, results))
    return pred, loss.reshape(()), grad_logits, grad_expr


def general_plan(logits, expr, spatial, slide_spots, spot_cells, cell_prior):
    place = lax.axis_index("spot")
    side = lax.axis_index("gene")
    rows_all = logits.shape[1]
    cell_rows = expr.shape[0]
    weights = cell_prior.astype(jnp.float32) / fixed_point
    gene_share = (place == 0).astype(jnp.float32)
    row_share = (side == 0).astype(jnp.float32)
    own_weights = lax.dynamic_slice_in_dim(weights, place * cell_rows, cell_rows, 0)
    expr_acc = jnp.zeros((cell_rows, expr.shape[1]), jnp.float32)
    loss_local = jnp.zeros((), jnp.float32)
    pred_list = []
    grad_list = []
    for slide in range(logits.shape[0]):
        logit_rows = logits[slide]
        counted = spot_cells[slide].astype(jnp.float32)
        target = spatial[slide]
        positions = place * rows_all + jnp.arange(rows_all, dtype=jnp.int32)
        valid = (positions < slide_spots[slide]).astype(jnp.float32)
        peak = jnp.max(logit_rows, axis=1, keepdims=True)
        raised = jnp.exp(logit_rows - peak)
        probs = raised / jnp.sum(raised, axis=1, keepdims=True)
        mass = jnp.dot(probs, weights, precision=lax.Precision.HIGHEST)
        blocks = lax.all_to_all(probs, "spot", split_axis=1, concat_axis=0, tiled=True)
        pred = lax.psum_scatter(
            jnp.dot(blocks, expr, precision=lax.Precision.HIGHEST),
            "spot",
            scatter_dimension=0,
            tiled=True,
        )
        gene_dot = jnp.sum(valid[:, None] * pred * target, axis=0)
        gene_pred = jnp.sum(valid[:, None] * pred * pred, axis=0)
        gene_true = jnp.sum(valid[:, None] * target * target, axis=0)
        mass_part = jnp.sum(valid * mass)
        kcell = valid * counted
        cell_part = jnp.sum(kcell)
        spot_dot = jnp.sum(pred * target, axis=1)
        spot_pred = jnp.sum(pred * pred, axis=1)
        spot_true = jnp.sum(target * target, axis=1)
        gene_dot, gene_pred, gene_true, mass_total, cell_total = lax.psum(
            (gene_dot, gene_pred, gene_true, mass_part, cell_part), "spot"
        )
        spot_dot, spot_pred, spot_true = lax.psum((spot_dot, spot_pred, spot_true), "gene")
        gene_inv = lax.rsqrt(gene_pred * gene_true + tiny)
        cos_gene = gene_dot * gene_inv
        spot_inv = lax.rsqrt(spot_pred * spot_true + tiny)
        cos_spot = spot_dot * spot_inv
        share = kcell / cell_total
        scale_count = slide_spots[slide].astype(jnp.float32)
        kl_part = jnp.sum(
            share * (jnp.log(counted) - jnp.log(cell_total) - jnp.log(mass) + jnp.log(mass_total))
        )
        loss_local = loss_local - gene_share * jnp.sum(cos_gene)
        loss_local = loss_local + row_share * (scale_count * kl_part - jnp.sum(valid * cos_spot))
        gene_back = cos_gene * gene_true / (gene_pred * gene_true + tiny)
        spot_back = cos_spot * spot_true / (spot_pred * spot_true + tiny)
        dpred = -valid[:, None] * (
            target * (gene_inv[None, :] + spot_inv[:, None])
            - pred * gene_back[None, :]
            - pred * spot_back[:, None]
        )
        dmass = scale_count * valid * (1.0 / mass_total - share / mass)
        pred_list.append(pred)
        grads_full, mass_full = (
            lax.all_gather(dpred, "spot", axis=0, tiled=True),
            lax.all_gather(dmass, "spot", axis=0, tiled=True),
        )
        dprob_cells = jnp.dot(grads_full, expr.T, precision=lax.Precision.HIGHEST)
        dprob_cells = lax.psum(dprob_cells, "gene")
        expr_acc = expr_acc + lax.dot_general(
            blocks, grads_full, (((0,), (0,)), ((), ())), precision=lax.Precision.HIGHEST
        )
        dprob_cells = dprob_cells + mass_full[:, None] * own_weights[None, :]
        dprob_rows = lax.all_to_all(dprob_cells, "spot", split_axis=0, concat_axis=1, tiled=True)
        inner = jnp.sum(probs * dprob_rows, axis=1, keepdims=True)
        dlogit = probs * (dprob_rows - inner)
        grad_list.append(dlogit)
    loss = lax.psum(loss_local, ("spot", "gene"))
    return (jnp.stack(pred_list), loss, jnp.stack(grad_list), expr_acc)


def solution(mesh):
    places = mesh.shape["spot"]

    def on_device(logits, expr, spatial, slide_spots, spot_cells, cell_prior):
        if places == PLANE * PLANE and mesh.shape["gene"] == 2 and expr.shape[1] == sum(FORWARD):
            return plane_call(
                logits, expr, spatial, slide_spots, spot_cells, cell_prior, places // PLANE
            )
        return general_plan(logits, expr, spatial, slide_spots, spot_cells, cell_prior)

    in_specs = (
        P(None, "spot", None),
        P("spot", "gene"),
        P(None, "spot", "gene"),
        P(),
        P(None, "spot"),
        P(),
    )
    out_specs = (P(None, "spot", "gene"), P(), P(None, "spot", None), P("spot", "gene"))
    return jax.shard_map(
        on_device, mesh=mesh, in_specs=in_specs, out_specs=out_specs, check_vma=False
    )
```

```python
import functools

import jax
import jax.numpy as jnp
from jax import lax
from jax.experimental import pallas as pl
from jax.experimental.pallas import tpu as pltpu
from jax.sharding import PartitionSpec as P

tiny = 1e-06
fixed_point = 16384.0
F32 = jnp.float32
BF16 = jnp.bfloat16
MESH = pl.DeviceIdType.MESH

PLANE = 4
LANES = 128
STEP_ROWS = 16
BLOCK = 32
TALL = 256
FORWARD = (128, 256, 256, 128, 128, 128)
BACKWARD = (128, 128, 256, 256, 256)
SPLIT = 4
LEAD = 1
NEAR_LEAD = 2
EARLY = 3
STEPS = (
    ("far", 0),
    ("near", 0),
    ("share",),
    ("far", 1),
    ("far", 2),
    ("far", 3),
    ("take",),
    ("whole", 0),
    ("near", 1),
    ("product", 0),
    ("sum", 0),
    ("whole", 1),
    ("near", 2),
    ("product", 1),
    ("whole", 2),
    ("product", 2),
    ("whole", 3),
    ("near", 3),
    ("product", 3),
    ("far", 4),
    ("whole", 4),
    ("near", 4),
    ("product", 4),
    ("sum", 1),
    ("turn", 0),
    ("far", 5),
    ("whole", 5),
    ("near", 5),
    ("product", 5),
    ("sum", 2),
    ("plane", 0),
    ("turn", 1),
    ("sum", 3),
    ("line", 0),
    ("sum", 4),
    ("sum", 5),
    ("cores",),
    ("plane", 1),
    ("genes", 0),
    ("spots",),
    ("grad", 0),
    ("grad", 1),
    ("grad", 2),
    ("line", 1),
    ("backward", 0),
    ("backward", 1),
    ("add_near", 0),
    ("genes", 1),
    ("grad", 3),
    ("backward", 2),
    ("probs", 0),
    ("add_far", 0),
    ("probs", 1),
    ("expr", 0),
    ("grad", 4),
    ("add_near", 1),
    ("probs", 2),
    ("terms",),
    ("backward", 3),
    ("probs", 3),
    ("add_near", 2),
    ("backward", 4),
    ("add_far", 1),
    ("probs", 4),
    ("exchange",),
    ("add_near", 3),
    ("add_far", 2),
    ("left",),
    ("return",),
    ("loss",),
    ("add_far", 3),
    ("expr", 1),
    ("add_near", 4),
    ("logits",),
    ("add_far", 4),
    ("expr", 2),
    ("expr", 3),
    ("expr", 4),
)


def halves(value):
    high = value.astype(BF16)
    return high, (value - high.astype(F32)).astype(BF16)


def threefold(value):
    high, low = halves(value)
    return jnp.concatenate([high, high, low], axis=1)


def product(a, b, contract):
    return lax.dot_general(a, b, (contract, ((), ())), preferred_element_type=F32)


def plane_kernel(lines, forward_widths, backward_widths, *refs):
    chunks, turns = len(forward_widths), len(backward_widths)
    (
        (logits_ref, expr_ref, spatial_ref, count_in, cells_in, prior_in),
        (pr, loss_ref, glog, ge),
        (count_ref, cells_ref, prior_ref, lg, lq, tg, ex, pq, ab, af, probs_3, turned_3, expr_3, sacc, s1, s2, gv, ss, rowv, rs),
        (grad_3, factor, t0, p0, vr, fs, fx, fy, fz, fr, inn, l1, l2),
        (loc, ou_s, ou_r, od_s, od_r, fu_s, fu_r, fd_s, fd_r, a_s, a_r, a2_s, a2_r, r_s, r_r),
        (c_s, c_r, s1_s, s1_r, s2_s, s2_r, ss_s, ss_r, d_s, d_r, ru_s, ru_r, rd_s, rd_r),
        (f_s, f_r, fx_s, fx_r, go_s, go_r, in_s, in_r, l1_s, l1_r, l2_s, l2_r, t0_s, t0_r, p0_s, p0_r, vr_s, vr_r),
        bb,
        cs,
        cr,
        ds,
        es,
        ru,
        rd,
    ) = grouped(refs, (6, 4, 20, 13, 15, 14, 18, chunks, chunks, chunks, turns, turns, turns, turns))
    place = lax.axis_index("spot")
    core = lax.axis_index("gene")
    z = place // PLANE
    q = place % PLANE
    col, row = q % 2, q // 2
    mates = ((1 - row) * 2 + 1 - col, row * 2 + 1 - col, (1 - row) * 2 + col)
    others = tuple((z + step) % lines for step in range(1, lines))
    up, down = (place + PLANE, core), (place - PLANE, core)
    sibling = (place, 1 - core)
    slides, slide_rows = logits_ref.shape[0], logits_ref.shape[1]
    rows = slides * slide_rows
    cb = expr_ref.shape[0]
    genes = expr_ref.shape[1]
    last = lines - 1

    def mate(p):
        return (z * PLANE + p, core)

    def send(src, dst, send_sem, recv_sem, device):
        copy = pltpu.make_async_remote_copy(
            src_ref=src, dst_ref=dst, send_sem=send_sem, recv_sem=recv_sem, device_id=device, device_id_type=MESH
        )
        copy.start()

    def arrived(dst, recv_sem):
        pltpu.make_async_copy(dst, dst, recv_sem).wait()

    sent = arrived

    def cols(k):
        return pl.ds(sum(forward_widths[:k]), forward_widths[k])

    def turn_cols(k):
        return pl.ds(sum(backward_widths[:k]), backward_widths[k])

    def block(index):
        return pl.ds(pl.multiple_of(index * cb, cb), cb)

    def share(index):
        return pl.ds(pl.multiple_of(index * rows, rows), rows)

    def half(index):
        return pl.ds(pl.multiple_of(index * slide_rows, slide_rows), slide_rows)

    small = ((prior_in, prior_ref), (count_in, count_ref), (cells_in, cells_ref))
    pltpu.make_async_copy(expr_ref, ex, loc.at[2 * slides]).start()
    for m in range(slides):
        pltpu.make_async_copy(logits_ref.at[m], lg.at[half(m)], loc.at[m]).start()
    for at, (src, dst) in enumerate(small):
        pltpu.make_async_copy(src, dst, loc.at[2 * slides + 1 + at]).start()
    for m in range(slides):
        pltpu.make_async_copy(spatial_ref.at[m], tg.at[half(m)], loc.at[slides + m]).start()

    barrier = pltpu.get_barrier_semaphore()
    for p in mates:
        pl.semaphore_signal(barrier, inc=1, device_id=mate(p), device_id_type=MESH)
    for o in others:
        pl.semaphore_signal(barrier, inc=1, device_id=(o * PLANE + q, core), device_id_type=MESH)
    pl.semaphore_signal(barrier, inc=1, device_id=sibling, device_id_type=MESH)
    pltpu.make_async_copy(expr_ref, ex, loc.at[2 * slides]).wait()
    for k in range(chunks):
        bb[k][block(z), :] = ex[:, cols(k)]
    for m in range(slides):
        pltpu.make_async_copy(logits_ref.at[m], lg.at[half(m)], loc.at[m]).wait()
    for p in range(PLANE):
        for line in range(lines):
            lq[p, :, pl.ds(line * cb, cb)] = lg[half(core), pl.ds((line * PLANE + p) * cb, cb)]
    pl.semaphore_wait(barrier, len(mates) + len(others) + 1)

    def own_up(k):
        here = bb[k].at[block(z)]
        send(here, here, ou_s.at[k], ou_r.at[k], up)

    def own_down(k):
        here = bb[k].at[block(z)]
        send(here, here, od_s.at[k], od_r.at[k], down)

    def low(at):
        return 2 * at < lines

    for at in range(lines):

        @pl.when(z == at)
        def _():
            for k in range(chunks):
                if at < last and (at == 0 or k < (LEAD if low(at) else NEAR_LEAD)):
                    own_up(k)
                if at > 0 and (at == last or k < (NEAR_LEAD if low(at) else LEAD)):
                    own_down(k)

    for p in mates:
        send(lq.at[p], ab.at[q, half(core)], a_s, a_r.at[q], mate(p))

    def from_below(k, at):
        arrived(bb[k].at[pl.ds((at - 1) * cb, cb)], ou_r.at[k])
        if at > 1:
            arrived(bb[k].at[pl.ds(0, (at - 1) * cb)], fu_r.at[k])

    def from_above(k, at):
        arrived(bb[k].at[pl.ds((at + 1) * cb, cb)], od_r.at[k])
        if at < last - 1:
            arrived(bb[k].at[pl.ds((at + 2) * cb, (last - 1 - at) * cb)], fd_r.at[k])

    def upward(k, at):
        from_below(k, at)
        here = bb[k].at[pl.ds(0, at * cb)]
        send(here, here, fu_s.at[k], fu_r.at[k], up)

    def downward(k, at):
        from_above(k, at)
        here = bb[k].at[pl.ds((at + 1) * cb, (last - at) * cb)]
        send(here, here, fd_s.at[k], fd_r.at[k], down)

    def forward_far(k):
        for at in range(1, last):

            @pl.when(z == at)
            def _():
                (upward if low(at) else downward)(k, at)
                if k + LEAD < chunks:
                    (own_up if low(at) else own_down)(k + LEAD)

    def forward_near(k):
        for at in range(1, last):

            @pl.when(z == at)
            def _():
                (downward if low(at) else upward)(k, at)
                if k + NEAR_LEAD < chunks:
                    (own_down if low(at) else own_up)(k + NEAR_LEAD)

    def gathered(k):
        @pl.when(z == 0)
        def _():
            from_above(k, 0)

        @pl.when(z == last)
        def _():
            from_below(k, last)

    for at, (src, dst) in enumerate(small):
        pltpu.make_async_copy(src, dst, loc.at[2 * slides + 1 + at]).wait()
    weights = prior_ref[...].astype(F32) / fixed_point

    @pl.loop(0, rows // STEP_ROWS)
    def _(step):
        at = pl.ds(pl.multiple_of(step * STEP_ROWS, STEP_ROWS), STEP_ROWS)
        value = lg[at, :]
        peak = jnp.max(value, axis=1, keepdims=True)
        raised = jnp.exp(value - peak)
        scale = 1.0 / jnp.sum(raised, axis=1, keepdims=True)
        probs = raised * scale
        mass_rows = jnp.sum(probs * weights, axis=1, keepdims=True)
        rowv[0, at, :] = jnp.broadcast_to(mass_rows, (STEP_ROWS, LANES))
        rowv[1, at, :] = jnp.broadcast_to(peak, (STEP_ROWS, LANES))
        rowv[2, at, :] = jnp.broadcast_to(scale, (STEP_ROWS, LANES))
        for p in range(PLANE):
            for line in range(lines):
                at_cells = (line * PLANE + p) * cb
                pq[p, at, pl.ds(line * cb, cb)] = probs[:, at_cells : at_cells + cb]

    wide = lax.broadcasted_iota(jnp.int32, (rows, LANES), 1)
    rs[q] = jnp.where(wide == 0, rowv[1], rowv[2]).T[0:8]
    for p in mates:
        send(rs.at[q], rs.at[q], r_s, r_r.at[q], mate(p))

    rid = lax.broadcasted_iota(jnp.int32, (rows, 1), 0)
    first = rid < slide_rows
    position = place * slide_rows + jnp.where(first, rid, rid - slide_rows)
    count = jnp.where(first, count_ref[0], count_ref[1])
    valid = (position < count).astype(F32)
    scale_count = count.astype(F32)
    square = (slide_rows, slide_rows)
    eye = lax.broadcasted_iota(jnp.int32, square, 0) == lax.broadcasted_iota(jnp.int32, square, 1)
    counted = jnp.concatenate(
        [
            jnp.sum(jnp.where(eye, cells_ref[m : m + 1, :].astype(F32), 0.0), axis=1, keepdims=True)
            for m in range(slides)
        ],
        axis=0,
    )
    mass = rowv[0, :, 0:1]
    kcell = valid * counted

    def by_slide(value):
        return [jnp.sum(value[m * slide_rows : (m + 1) * slide_rows], axis=0, keepdims=True) for m in range(slides)]

    mass_parts = by_slide(valid * mass)
    cell_parts = by_slide(kcell)
    lane = lax.broadcasted_iota(jnp.int32, (1, LANES), 1)
    scalars = jnp.zeros((1, LANES), F32)
    for at, value in enumerate(mass_parts + cell_parts):
        scalars = jnp.where(lane == at, value, scalars)
    for m in range(slides):
        pltpu.make_async_copy(spatial_ref.at[m], tg.at[half(m)], loc.at[slides + m]).wait()

    head = backward_widths[0]
    t0[q] = tg[:, 0:head]
    for p in mates:
        send(t0.at[q], t0.at[q], t0_s, t0_r.at[q], mate(p))
    sacc[...] = jnp.zeros_like(sacc)
    s1[q, 3 * slides :, :] = jnp.zeros((8 - 3 * slides, genes), F32)
    s1[q, 3 * slides : 3 * slides + 1, 0:LANES] = scalars

    def share_logits():
        for p in (mates[1], mates[2], mates[0]):
            here = ab.at[p, half(core)]
            arrived(here, a_r.at[p])
            send(here, here, a2_s, a2_r.at[p], sibling)

    def lay_probs(p, at, value):
        af[p, at, :] = value
        there = pl.ds(pl.multiple_of(p * rows + at.start, BLOCK), BLOCK)
        probs_3[there, :] = threefold(value)

    def take_probs():
        in_blocks(0, rows, lambda at: lay_probs(q, at, pq[q, at, :]))
        for p in (mates[1], mates[2], mates[0]):
            arrived(rs.at[p], r_r.at[p])
            arrived(ab.at[p, half(1 - core)], a2_r.at[p])
            rowv[1] = jnp.concatenate([rs[p].T, jnp.zeros((rows, LANES - 8), F32)], axis=1)

            def take(at):
                probs = jnp.exp(ab[p, at, :] - rowv[1, at, 0:1]) * rowv[1, at, 1:2]
                lay_probs(p, at, probs)

            in_blocks(0, rows, take)

    def transpose(part):
        @pl.loop(0, PLANE // 2)
        def _(step):
            p = part * (PLANE // 2) + step
            high, low_part = halves(af[p].T)
            for third, value in enumerate((high, high, low_part)):
                turned_3[:, pl.ds(pl.multiple_of(third * PLANE * rows + p * rows, rows), rows)] = value

    def in_blocks(start, count, body):
        @pl.loop(0, count // BLOCK)
        def _(step):
            body(pl.ds(pl.multiple_of(start + step * BLOCK, BLOCK), BLOCK))

    quarter = lines * cb

    def lay_factor(at, length, width, value):
        high, low_part = halves(value)
        for third, part in enumerate((high, low_part, high)):
            here = pl.ds(pl.multiple_of(third * length + at.start, BLOCK), BLOCK)
            factor[here, 0:width] = part

    def keep_expr(k, at, value):
        start = sum(forward_widths[:k])
        for turn in range(turns):
            origin, width = sum(backward_widths[:turn]), backward_widths[turn]
            lo, hi = max(start, origin), min(start + forward_widths[k], origin + width)
            if lo < hi:
                high, low_part = halves(value[:, lo - start : hi - start])
                for third, part in enumerate((high, low_part, high)):
                    expr_3[at, pl.ds(3 * origin + third * width + lo - origin, hi - lo)] = part

    def three_turn_cols(k):
        return pl.ds(3 * sum(backward_widths[:k]), 3 * backward_widths[k])

    def forward_product(k):
        width = forward_widths[k]

        def lay(at):
            value = bb[k][at, :]
            lay_factor(at, quarter, width, value)
            keep_expr(k, at, value)

        in_blocks(0, quarter, lay)
        if k < chunks - 1:

            @pl.loop(0, PLANE * rows // TALL)
            def _(step):
                tall = pl.ds(pl.multiple_of(step * TALL, TALL), TALL)
                cs[k][tall, :] = product(probs_3[tall, :], factor[0 : 3 * quarter, 0:width], ((1,), (0,)))

            for p in mates:
                pass_pred(k, p)
        else:
            for side, served in ((1 - row, (mates[0], mates[2])), (row, (mates[1],))):
                pair = pl.ds(pl.multiple_of(2 * side * rows, 2 * rows), 2 * rows)
                cs[k][pair, :] = product(probs_3[pair, :], factor[0 : 3 * quarter, 0:width], ((1,), (0,)))
                for p in served:
                    pass_pred(k, p)

    def pass_pred(k, p):
        send(cs[k].at[share(p)], cr[k].at[q], c_s.at[k], c_r.at[k, q], mate(p))

    def finish_pred(k):
        total = cs[k][share(q), :]
        for p in mates:
            arrived(cr[k].at[p], c_r.at[k, p])
            total = total + cr[k][p]
        pr[:, cols(k)] = total
        if k == 0:
            p0[q] = total[:, 0:head]
            for p in mates:
                send(p0.at[q], p0.at[q], p0_s, p0_r.at[q], mate(p))
        truth = tg[:, cols(k)]
        for at, value in enumerate((total * truth, total * total, truth * truth)):
            sacc[at] += lane_groups(value)
        kept = valid * total
        stats = by_slide(kept * truth) + by_slide(kept * total) + by_slide(valid * truth * truth)
        s1[q, 0 : 3 * slides, cols(k)] = jnp.concatenate(stats, axis=0)

    early = sum(forward_widths[:EARLY])
    parts = (pl.ds(0, early), pl.ds(early, genes - early))

    def sum_plane(at):
        for p in mates:
            send(s1.at[q, :, parts[at]], s1.at[q, :, parts[at]], s1_s, s1_r.at[at, q], mate(p))

    def sum_line(at):
        for p in mates:
            arrived(s1.at[p, :, parts[at]], s1_r.at[at, p])
        s2[z, :, parts[at]] = (s1[0, :, parts[at]] + s1[1, :, parts[at]]) + (s1[2, :, parts[at]] + s1[3, :, parts[at]])
        for o in others:
            send(s2.at[z, :, parts[at]], s2.at[z, :, parts[at]], s2_s, s2_r.at[at, z], (o * PLANE + q, core))

    kept = {}

    def finish_genes(at):
        for o in others:
            arrived(s2.at[o, :, parts[at]], s2_r.at[at, o])
        total = s2[0, :, parts[at]]
        for line in range(1, lines):
            total = total + s2[line, :, parts[at]]
        gene_dot, gene_pred, gene_true = total[0:2], total[2:4], total[4:6]
        gene_inv = lax.rsqrt(gene_pred * gene_true + tiny)
        cos_gene = gene_dot * gene_inv
        gv[0:2, parts[at]] = gene_inv
        gv[2:4, parts[at]] = cos_gene * gene_true / (gene_pred * gene_true + tiny)
        kept["genes", at] = jnp.sum(jnp.sum(cos_gene, axis=1, keepdims=True), axis=0, keepdims=True)
        if at == 0:
            kept["mass"] = jnp.where(first, total[6:7, 0:1], total[6:7, 1:2])
            kept["cells"] = jnp.where(first, total[6:7, 2:3], total[6:7, 3:4])

    def sum_cores():
        sums = [jnp.sum(sacc[at], axis=1, keepdims=True) for at in range(3)]
        ss[core] = jnp.where(wide == 0, sums[0], jnp.where(wide == 1, sums[1], sums[2])).T[0:8]
        send(ss.at[core], ss.at[core], ss_s, ss_r, sibling)

    def finish_spots():
        lane_id = lax.broadcasted_iota(jnp.int32, (1, rows), 1)
        first_lane = lane_id < slide_rows
        lane_position = place * slide_rows + jnp.where(first_lane, lane_id, lane_id - slide_rows)
        lane_valid = (lane_position < jnp.where(first_lane, count_ref[0], count_ref[1])).astype(F32)
        arrived(ss.at[1 - core], ss_r)
        spot = ss[0] + ss[1]
        spot_dot, spot_pred, spot_true = spot[0:1], spot[1:2], spot[2:3]
        spot_inv = lax.rsqrt(spot_pred * spot_true + tiny)
        cos_spot = spot_dot * spot_inv
        spot_back = cos_spot * spot_true / (spot_pred * spot_true + tiny)
        kept["cos"] = jnp.sum(lane_valid * cos_spot, axis=1, keepdims=True)
        vectors = [lane_valid * spot_inv, lane_valid * spot_back, lane_valid, jnp.zeros((5, rows), F32)]
        vr[q] = jnp.concatenate(vectors, axis=0)
        sacc[0] = jnp.zeros_like(sacc[0])

    def gradient(truth, guess, by_row, k):
        pieces = []
        for m in range(slides):
            lo, hi = m * slide_rows, (m + 1) * slide_rows
            inverse, back = gv[m : m + 1, turn_cols(k)], gv[2 + m : 3 + m, turn_cols(k)]
            spot_inv, spot_back, spot_valid = by_row[lo:hi, 0:1], by_row[lo:hi, 1:2], by_row[lo:hi, 2:3]
            pieces.append(
                guess[lo:hi] * (spot_valid * back + spot_back) - truth[lo:hi] * (spot_valid * inverse + spot_inv)
            )
        return jnp.concatenate(pieces, axis=0)

    def head_gradient():
        for p in mates:
            arrived(t0.at[p], t0_r.at[p])
            arrived(p0.at[p], p0_r.at[p])
            arrived(vr.at[p], vr_r.at[p])
        for p in range(PLANE):
            ds[0][share(p), :] = gradient(t0[p], p0[p], vr[p].T, 0)
        sacc[0] += lane_groups(ds[0][share(q), :] * p0[q])

    def send_grad(k):
        if k == 0:
            for p in mates:
                send(vr.at[q], vr.at[q], vr_s, vr_r.at[q], mate(p))
            kept["by_row"] = vr[q].T
            return
        grad = gradient(tg[:, turn_cols(k)], pr[:, turn_cols(k)], kept["by_row"], k)
        here = ds[k].at[share(q)]
        here[...] = grad
        for p in mates:
            send(here, here, d_s.at[k], d_r.at[k, q], mate(p))
        sacc[0] += lane_groups(grad * pr[:, turn_cols(k)])

    def send_terms():
        mass_total, cell_total = kept["mass"], kept["cells"]
        portion = kcell / cell_total
        kl_rows = portion * (jnp.log(counted) - jnp.log(cell_total) - jnp.log(mass) + jnp.log(mass_total))
        dmass = scale_count * valid * (1.0 / mass_total - portion / mass)
        terms = jnp.sum(scale_count * kl_rows, axis=0, keepdims=True) - kept["cos"]
        l1[q] = jnp.broadcast_to(terms, (8, LANES))
        for p in mates:
            send(l1.at[q], l1.at[q], l1_s, l1_r.at[q], mate(p))
        inner = jnp.sum(sacc[0], axis=1, keepdims=True)
        inn[core] = jnp.where(wide == 0, inner, kept["genes", 0] + kept["genes", 1])
        send(inn.at[core], inn.at[core], in_s, in_r, sibling)
        rowv[1] = jnp.broadcast_to(dmass, (rows, LANES))

    middle = lines // 2

    def backward_product(k):
        if k == 0:
            head_gradient()
        else:
            for p in mates:
                arrived(ds[k].at[share(p)], d_r.at[k, p])
        width, spots = backward_widths[k], PLANE * rows

        def lay(at):
            value = ds[k][at, :]
            lay_factor(at, spots, width, value)
            grad_3[at, three_turn_cols(k)] = threefold(value)

        in_blocks(0, spots, lay)
        if not halved(k):

            @pl.loop(0, quarter // TALL)
            def _(step):
                tall = pl.ds(pl.multiple_of(step * TALL, TALL), TALL)
                es[k][tall, :] = product(turned_3[tall, :], factor[0 : 3 * spots, 0:width], ((1,), (0,)))

        for turn in range(2):
            if halved(k):
                side = (1 - z // middle) if turn == 0 else z // middle
                pair = pl.ds(pl.multiple_of(side * middle * cb, middle * cb), middle * cb)
                es[k][pair, :] = product(turned_3[pair, :], factor[0 : 3 * spots, 0:width], ((1,), (0,)))

            @pl.when(z == 0)
            def _():
                if halved(k):
                    pass_up(k, middle if turn == 0 else 1, middle if turn == 0 else middle - 1, turn)
                elif whole(k):
                    if turn == 0:
                        pass_up(k, 1, last, 0)
                elif turn == 0:
                    for line in range(last, 0, -1):
                        pass_up(k, line, 1, line)

            @pl.when(z == last)
            def _():
                if halved(k):
                    pass_down(k, 0 if turn == 0 else middle, middle if turn == 0 else middle - 1, turn)
                elif whole(k):
                    if turn == 0:
                        pass_down(k, 0, last, 0)
                elif turn == 0:
                    for line in range(last):
                        pass_down(k, line, 1, line)

    def halved(k):
        return k == 0

    def whole(k):
        return 0 < k < turns - SPLIT

    def pass_up(k, line, count, slot):
        here = pl.ds(line * cb, count * cb)
        send(es[k].at[here], ru[k].at[here], ru_s.at[k], ru_r.at[k, slot], up)

    def pass_down(k, line, count, slot):
        here = pl.ds(line * cb, count * cb)
        send(es[k].at[here], rd[k].at[here], rd_s.at[k], rd_r.at[k, slot], down)

    def take_up(k, line, count, slot):
        arrived(ru[k].at[pl.ds(line * cb, count * cb)], ru_r.at[k, slot])

    def take_down(k, line, count, slot):
        arrived(rd[k].at[pl.ds(line * cb, count * cb)], rd_r.at[k, slot])

    def add_up(k, line, count):
        def add(at):
            es[k][at, :] += ru[k][at, :]

        in_blocks(line * cb, count * cb, add)

    def add_down(k, line, count):
        def add(at):
            es[k][at, :] += rd[k][at, :]

        in_blocks(line * cb, count * cb, add)

    def rising(k, at):
        if halved(k) or whole(k):
            start = middle if halved(k) else at
            take_up(k, start, lines - start, 0)
            above = max(at + 1, start)
            add_up(k, above, lines - above)
            pass_up(k, above, lines - above, 0)
        else:
            for line in range(last, at, -1):
                take_up(k, line, 1, line)
                add_up(k, line, 1)
                pass_up(k, line, 1, line)

    def falling(k, at):
        if halved(k) or whole(k):
            end = middle if halved(k) else at + 1
            take_down(k, 0, end, 0)
            below = min(at, end)
            add_down(k, 0, below)
            pass_down(k, 0, below, 0)
        else:
            for line in range(at):
                take_down(k, line, 1, line)
                add_down(k, line, 1)
                pass_down(k, line, 1, line)

    def add_near(k):
        for at in range(1, last):

            @pl.when(z == at)
            def _():
                (rising if low(at) else falling)(k, at)

    def add_far(k):
        for at in range(1, last):

            @pl.when(z == at)
            def _():
                (falling if low(at) else rising)(k, at)

    def finish_expr(k):
        for at in range(lines):

            @pl.when(z == at)
            def _():
                if at > 0:
                    if halved(k) and at < middle:
                        take_up(k, at, 1, 1)
                    elif at == last and (halved(k) or whole(k)):
                        take_up(k, at, 1, 0)
                    elif not halved(k) and not whole(k):
                        take_up(k, at, 1, at)
                if at < last:
                    if halved(k) and at >= middle:
                        take_down(k, at, 1, 1)
                    elif at == 0 and (halved(k) or whole(k)):
                        take_down(k, at, 1, 0)
                    elif not halved(k) and not whole(k):
                        take_down(k, at, 1, at)

        from_low, from_high = z > 0, z < last

        @pl.loop(0, cb // BLOCK)
        def _(step):
            here = pl.ds(pl.multiple_of(step * BLOCK, BLOCK), BLOCK)
            own = pl.ds(pl.multiple_of(z * cb + step * BLOCK, BLOCK), BLOCK)
            total = es[k][own, :]
            total = total + jnp.where(from_low, ru[k][own, :], 0.0)
            ge[here, turn_cols(k)] = total + jnp.where(from_high, rd[k][own, :], 0.0)

    def probs_gradient(k):
        at = three_turn_cols(k)

        @pl.loop(0, PLANE * rows // TALL)
        def _(step):
            tall = pl.ds(pl.multiple_of(step * TALL, TALL), TALL)
            part = product(grad_3[tall, at], expr_3[:, at], ((1,), (1,)))
            if k == 0:
                fs[tall, :] = part
            else:
                fs[tall, :] += part

    def slide_of(p, m):
        return pl.ds(pl.multiple_of(p * rows + m * slide_rows, slide_rows), slide_rows)

    def sum_probs_cores():
        for p in mates + (q,):
            fx[p] = fs[slide_of(p, 1 - core), :]
            send(fx.at[p], fy.at[p], fx_s, fx_r.at[p], sibling)

    def return_probs():
        for p in mates:
            arrived(fy.at[p], fx_r.at[p])
            fz[p] = fs[slide_of(p, core), :] + fy[p]
            send(fz.at[p], fr.at[q], f_s, f_r.at[q], mate(p))
        arrived(fy.at[q], fx_r.at[q])
        fr[q] = fs[slide_of(q, core), :] + fy[q]

    def pass_terms():
        for p in mates:
            arrived(l1.at[p], l1_r.at[p])
        l2[z] = (l1[0] + l1[1]) + (l1[2] + l1[3])
        for o in others:
            send(l2.at[z], l2.at[z], l2_s, l2_r.at[z], (o * PLANE + q, core))

    def part_of(slide, m):
        start = slide * slide_rows + m * (slide_rows // 2)
        return pl.ds(pl.multiple_of(start, slide_rows // 2), slide_rows // 2)

    def finish_logits():
        arrived(inn.at[1 - core], in_r)
        rowv[2] = (inn[0] + inn[1]) + rowv[1] * rowv[0]
        for p in mates:
            arrived(fr.at[p], f_r.at[p])
        for m in range(2):

            @pl.loop(0, slide_rows // STEP_ROWS // 2)
            def _(step):
                row_at = (m * (slide_rows // STEP_ROWS // 2) + step) * STEP_ROWS
                at = pl.ds(pl.multiple_of(row_at, STEP_ROWS), STEP_ROWS)
                whole_at = pl.ds(pl.multiple_of(core * slide_rows + row_at, STEP_ROWS), STEP_ROWS)
                by_mass, total_inner = rowv[1, whole_at, 0:1], rowv[2, whole_at, 0:1]
                for p in range(PLANE):
                    for line in range(lines):
                        here, there = pl.ds(line * cb, cb), (line * PLANE + p) * cb
                        grad = fr[p, at, here] + by_mass * weights[:, there : there + cb]
                        glog[whole_at, pl.ds(there, cb)] = pq[p, whole_at, here] * (grad - total_inner)

            here = part_of(core, m)
            send(glog.at[here], glog.at[here], go_s, go_r.at[m], sibling)

    def forward_left():
        for k in range(chunks):

            @pl.when(z < last)
            def _():
                sent(bb[k].at[block(z)], ou_s.at[k])

            @pl.when(z > 0)
            def _():
                sent(bb[k].at[block(z)], od_s.at[k])

            for at in range(1, last):

                @pl.when(z == at)
                def _():
                    sent(bb[k].at[pl.ds(0, at * cb)], fu_s.at[k])
                    sent(bb[k].at[pl.ds((at + 1) * cb, (last - at) * cb)], fd_s.at[k])

        three = pl.ds(0, len(mates))
        sent(ab.at[three, half(0)], a_s)
        sent(ab.at[three, half(0)], a2_s)
        sent(rs.at[three], r_s)
        sent(t0.at[three], t0_s)
        sent(p0.at[three], p0_s)
        for k in range(chunks):
            sent(cr[k].at[three], c_s.at[k])
        sent(s1.at[three], s1_s)
        sent(s2.at[pl.ds(0, last)], s2_s)
        sent(ss.at[0], ss_s)

    steps = {
        "far": forward_far,
        "near": forward_near,
        "share": share_logits,
        "take": take_probs,
        "whole": gathered,
        "product": forward_product,
        "sum": finish_pred,
        "turn": transpose,
        "plane": sum_plane,
        "line": sum_line,
        "genes": finish_genes,
        "cores": sum_cores,
        "spots": finish_spots,
        "grad": send_grad,
        "terms": send_terms,
        "backward": backward_product,
        "probs": probs_gradient,
        "exchange": sum_probs_cores,
        "return": return_probs,
        "loss": pass_terms,
        "logits": finish_logits,
        "add_near": add_near,
        "add_far": add_far,
        "expr": finish_expr,
        "left": forward_left,
    }
    for name, *where in STEPS:
        steps[name](*where)

    for o in others:
        arrived(l2.at[o], l2_r.at[o])
    loss = l2[0]
    for line in range(1, lines):
        loss = loss + l2[line]
    loss_ref[...] = loss[0:1, 0:1] - (inn[0, 0:1, 1:2] + inn[1, 0:1, 1:2])
    for m in range(2):
        arrived(glog.at[part_of(1 - core, m)], go_r.at[m])

    for k in range(turns):
        for at in range(lines):

            @pl.when(z == at)
            def _():
                if at < last:
                    sent(es[k].at[pl.ds((at + 1) * cb, (last - at) * cb)], ru_s.at[k])
                if at > 0:
                    sent(es[k].at[pl.ds(0, at * cb)], rd_s.at[k])

    three = pl.ds(0, len(mates))
    for k in range(1, turns):
        sent(ds[k].at[pl.ds(0, len(mates) * rows)], d_s.at[k])
    sent(vr.at[three], vr_s)
    sent(inn.at[0], in_s)
    sent(l1.at[three], l1_s)
    sent(l2.at[pl.ds(0, last)], l2_s)
    sent(fr.at[three], f_s)
    sent(fx, fx_s)
    sent(glog.at[half(0)], go_s)


def lane_groups(value):
    parts = [value[:, at : at + LANES] for at in range(0, value.shape[1], LANES)]
    return functools.reduce(lambda a, b: a + b, parts)


def grouped(refs, sizes):
    at = 0
    for size in sizes:
        yield refs[at : at + size]
        at += size


def deliver(pred_in, loss_in, glog_in, gexp_in, pred_ref, loss_ref, glog_ref, gexp_ref, sems):
    slides, slide_rows = pred_ref.shape[0], pred_ref.shape[1]
    pairs = [(gexp_in, gexp_ref), (loss_in, loss_ref)]
    for m in range(slides):
        part = pl.ds(m * slide_rows, slide_rows)
        pairs += [(glog_in.at[part], glog_ref.at[m]), (pred_in.at[part], pred_ref.at[m])]
    copies = [pltpu.make_async_copy(src, dst, sems.at[at]) for at, (src, dst) in enumerate(pairs)]
    for copy in copies:
        copy.start()
    for copy in copies:
        copy.wait()


def plane_call(logits, expr, spatial, slide_spots, spot_cells, cell_prior, lines):
    slides, slide_rows, cells = logits.shape
    rows = slides * slide_rows
    cb, genes = expr.shape
    quarter = lines * cb
    spots = PLANE * rows
    chunks, turns = len(FORWARD), len(BACKWARD)
    dma = pltpu.SemaphoreType.DMA
    vmem = pltpu.VMEM
    anywhere = pl.BlockSpec(memory_space=pl.ANY)
    in_vmem = pl.BlockSpec(memory_space=pltpu.VMEM)
    scratch = [
        pltpu.SMEM((slides,), jnp.int32),
        vmem((slides, slide_rows), jnp.int32),
        vmem((1, cells), jnp.int32),
        vmem((rows, cells), F32),
        vmem((PLANE, slide_rows, quarter), F32),
        vmem((rows, genes), F32),
        vmem((cb, genes), F32),
        vmem((PLANE, rows, quarter), F32),
        vmem((PLANE, rows, quarter), F32),
        vmem((PLANE, rows, quarter), F32),
        vmem((spots, 3 * quarter), BF16),
        vmem((quarter, 3 * spots), BF16),
        vmem((quarter, 3 * genes), BF16),
        vmem((3, rows, LANES), F32),
        vmem((PLANE, 8, genes), F32),
        vmem((lines, 8, genes), F32),
        vmem((8, genes), F32),
        vmem((2, 8, rows), F32),
        vmem((3, rows, LANES), F32),
        vmem((PLANE, 8, rows), F32),
        vmem((spots, 3 * genes), BF16),
        vmem((3 * max(quarter, spots), max(FORWARD + BACKWARD)), BF16),
        vmem((PLANE, rows, BACKWARD[0]), F32),
        vmem((PLANE, rows, BACKWARD[0]), F32),
        vmem((PLANE, 8, rows), F32),
        vmem((spots, quarter), F32),
        vmem((PLANE, slide_rows, quarter), F32),
        vmem((PLANE, slide_rows, quarter), F32),
        vmem((PLANE, slide_rows, quarter), F32),
        vmem((PLANE, slide_rows, quarter), F32),
        vmem((2, rows, LANES), F32),
        vmem((PLANE, 8, LANES), F32),
        vmem((lines, 8, LANES), F32),
        dma((2 * slides + 4,)),
        dma((chunks,)),
        dma((chunks,)),
        dma((chunks,)),
        dma((chunks,)),
        dma((chunks,)),
        dma((chunks,)),
        dma((chunks,)),
        dma((chunks,)),
        dma,
        dma((PLANE,)),
        dma,
        dma((PLANE,)),
        dma,
        dma((PLANE,)),
        dma((chunks,)),
        dma((chunks, PLANE)),
        dma,
        dma((2, PLANE)),
        dma,
        dma((2, lines)),
        dma,
        dma,
        dma((turns,)),
        dma((turns, PLANE)),
        dma((turns,)),
        dma((turns, lines)),
        dma((turns,)),
        dma((turns, lines)),
        dma,
        dma((PLANE,)),
        dma,
        dma((PLANE,)),
        dma,
        dma((2,)),
        dma,
        dma,
        dma,
        dma((PLANE,)),
        dma,
        dma((lines,)),
        dma,
        dma((PLANE,)),
        dma,
        dma((PLANE,)),
        dma,
        dma((PLANE,)),
    ]
    for shape, widths in (
        ((quarter,), FORWARD),
        ((spots,), FORWARD),
        ((PLANE, rows), FORWARD),
        ((spots,), BACKWARD),
        ((quarter,), BACKWARD),
        ((quarter,), BACKWARD),
        ((quarter,), BACKWARD),
    ):
        scratch += [vmem(shape + (width,), F32) for width in widths]
    in_hbm = functools.partial(pltpu.with_memory_space_constraint, memory_space=pltpu.HBM)
    in_place = functools.partial(pltpu.with_memory_space_constraint, memory_space=pltpu.VMEM)
    results = pl.pallas_call(
        functools.partial(plane_kernel, lines, FORWARD, BACKWARD),
        out_shape=(
            vmem((rows, genes), F32),
            vmem((1, 1), F32),
            vmem((rows, cells), F32),
            vmem((cb, genes), F32),
        ),
        in_specs=[anywhere] * 6,
        out_specs=(in_vmem,) * 4,
        scratch_shapes=scratch,
        compiler_params=pltpu.CompilerParams(
            collective_id=0, has_side_effects=True, vmem_limit_bytes=48 * 1024 * 1024
        ),
    )(*map(in_hbm, (logits, expr, spatial, slide_spots, spot_cells, cell_prior.reshape(1, cells))))
    pred, loss, grad_logits, grad_expr = pl.pallas_call(
        deliver,
        out_shape=(
            jax.ShapeDtypeStruct((slides, slide_rows, genes), F32),
            jax.ShapeDtypeStruct((1, 1), F32),
            jax.ShapeDtypeStruct((slides, slide_rows, cells), F32),
            jax.ShapeDtypeStruct((cb, genes), F32),
        ),
        in_specs=[anywhere] * 4,
        out_specs=(anywhere,) * 4,
        scratch_shapes=[dma((2 * slides + 2,))],
        compiler_params=pltpu.CompilerParams(vmem_limit_bytes=4 * 1024 * 1024),
    )(*map(in_place, results))
    return pred, loss.reshape(()), grad_logits, grad_expr


def general_plan(logits, expr, spatial, slide_spots, spot_cells, cell_prior):
    place = lax.axis_index("spot")
    side = lax.axis_index("gene")
    rows_all = logits.shape[1]
    cell_rows = expr.shape[0]
    weights = cell_prior.astype(jnp.float32) / fixed_point
    gene_share = (place == 0).astype(jnp.float32)
    row_share = (side == 0).astype(jnp.float32)
    own_weights = lax.dynamic_slice_in_dim(weights, place * cell_rows, cell_rows, 0)
    expr_acc = jnp.zeros((cell_rows, expr.shape[1]), jnp.float32)
    loss_local = jnp.zeros((), jnp.float32)
    pred_list = []
    grad_list = []
    for slide in range(logits.shape[0]):
        logit_rows = logits[slide]
        counted = spot_cells[slide].astype(jnp.float32)
        target = spatial[slide]
        positions = place * rows_all + jnp.arange(rows_all, dtype=jnp.int32)
        valid = (positions < slide_spots[slide]).astype(jnp.float32)
        peak = jnp.max(logit_rows, axis=1, keepdims=True)
        raised = jnp.exp(logit_rows - peak)
        probs = raised / jnp.sum(raised, axis=1, keepdims=True)
        mass = jnp.dot(probs, weights, precision=lax.Precision.HIGHEST)
        blocks = lax.all_to_all(probs, "spot", split_axis=1, concat_axis=0, tiled=True)
        pred = lax.psum_scatter(
            jnp.dot(blocks, expr, precision=lax.Precision.HIGHEST),
            "spot",
            scatter_dimension=0,
            tiled=True,
        )
        gene_dot = jnp.sum(valid[:, None] * pred * target, axis=0)
        gene_pred = jnp.sum(valid[:, None] * pred * pred, axis=0)
        gene_true = jnp.sum(valid[:, None] * target * target, axis=0)
        mass_part = jnp.sum(valid * mass)
        kcell = valid * counted
        cell_part = jnp.sum(kcell)
        spot_dot = jnp.sum(pred * target, axis=1)
        spot_pred = jnp.sum(pred * pred, axis=1)
        spot_true = jnp.sum(target * target, axis=1)
        gene_dot, gene_pred, gene_true, mass_total, cell_total = lax.psum(
            (gene_dot, gene_pred, gene_true, mass_part, cell_part), "spot"
        )
        spot_dot, spot_pred, spot_true = lax.psum((spot_dot, spot_pred, spot_true), "gene")
        gene_inv = lax.rsqrt(gene_pred * gene_true + tiny)
        cos_gene = gene_dot * gene_inv
        spot_inv = lax.rsqrt(spot_pred * spot_true + tiny)
        cos_spot = spot_dot * spot_inv
        share = kcell / cell_total
        scale_count = slide_spots[slide].astype(jnp.float32)
        kl_part = jnp.sum(
            share * (jnp.log(counted) - jnp.log(cell_total) - jnp.log(mass) + jnp.log(mass_total))
        )
        loss_local = loss_local - gene_share * jnp.sum(cos_gene)
        loss_local = loss_local + row_share * (scale_count * kl_part - jnp.sum(valid * cos_spot))
        gene_back = cos_gene * gene_true / (gene_pred * gene_true + tiny)
        spot_back = cos_spot * spot_true / (spot_pred * spot_true + tiny)
        dpred = -valid[:, None] * (
            target * (gene_inv[None, :] + spot_inv[:, None])
            - pred * gene_back[None, :]
            - pred * spot_back[:, None]
        )
        dmass = scale_count * valid * (1.0 / mass_total - share / mass)
        pred_list.append(pred)
        grads_full, mass_full = (
            lax.all_gather(dpred, "spot", axis=0, tiled=True),
            lax.all_gather(dmass, "spot", axis=0, tiled=True),
        )
        dprob_cells = jnp.dot(grads_full, expr.T, precision=lax.Precision.HIGHEST)
        dprob_cells = lax.psum(dprob_cells, "gene")
        expr_acc = expr_acc + lax.dot_general(
            blocks, grads_full, (((0,), (0,)), ((), ())), precision=lax.Precision.HIGHEST
        )
        dprob_cells = dprob_cells + mass_full[:, None] * own_weights[None, :]
        dprob_rows = lax.all_to_all(dprob_cells, "spot", split_axis=0, concat_axis=1, tiled=True)
        inner = jnp.sum(probs * dprob_rows, axis=1, keepdims=True)
        dlogit = probs * (dprob_rows - inner)
        grad_list.append(dlogit)
    loss = lax.psum(loss_local, ("spot", "gene"))
    return (jnp.stack(pred_list), loss, jnp.stack(grad_list), expr_acc)


def solution(mesh):
    places = mesh.shape["spot"]

    def on_device(logits, expr, spatial, slide_spots, spot_cells, cell_prior):
        if places == PLANE * PLANE and mesh.shape["gene"] == 2 and expr.shape[1] == sum(FORWARD):
            return plane_call(
                logits, expr, spatial, slide_spots, spot_cells, cell_prior, places // PLANE
            )
        return general_plan(logits, expr, spatial, slide_spots, spot_cells, cell_prior)

    in_specs = (
        P(None, "spot", None),
        P("spot", "gene"),
        P(None, "spot", "gene"),
        P(),
        P(None, "spot"),
        P(),
    )
    out_specs = (P(None, "spot", "gene"), P(), P(None, "spot", None), P("spot", "gene"))
    return jax.shard_map(
        on_device, mesh=mesh, in_specs=in_specs, out_specs=out_specs, check_vma=False
    )
```

```python
import functools

import jax
import jax.numpy as jnp
from jax import lax
from jax.experimental import pallas as pl
from jax.experimental.pallas import tpu as pltpu
from jax.sharding import PartitionSpec as P

tiny = 1e-06
fixed_point = 16384.0
F32 = jnp.float32
BF16 = jnp.bfloat16
MESH = pl.DeviceIdType.MESH

PLANE = 4
LANES = 128
STEP_ROWS = 16
BLOCK = 32
TALL = 256
FORWARD = (128, 256, 256, 128, 128, 128)
BACKWARD = (128, 256, 256, 256, 128)
SPLIT = 4
LEAD = 1
NEAR_LEAD = 2
EARLY = 3
STEPS = (
    ("far", 0),
    ("far", 1),
    ("near", 0),
    ("share",),
    ("far", 2),
    ("far", 3),
    ("take",),
    ("whole", 0),
    ("near", 1),
    ("product", 0),
    ("sum", 0),
    ("whole", 1),
    ("near", 2),
    ("product", 1),
    ("whole", 2),
    ("product", 2),
    ("whole", 3),
    ("near", 3),
    ("product", 3),
    ("far", 4),
    ("whole", 4),
    ("near", 4),
    ("product", 4),
    ("sum", 1),
    ("turn", 0),
    ("far", 5),
    ("whole", 5),
    ("near", 5),
    ("product", 5),
    ("sum", 2),
    ("plane", 0),
    ("turn", 1),
    ("sum", 3),
    ("line", 0),
    ("sum", 4),
    ("sum", 5),
    ("plane", 1),
    ("cores",),
    ("genes", 0),
    ("spots",),
    ("grad", 0),
    ("grad", 1),
    ("grad", 2),
    ("line", 1),
    ("backward", 0),
    ("backward", 1),
    ("add_near", 0),
    ("genes", 1),
    ("grad", 3),
    ("backward", 2),
    ("probs", 0),
    ("add_far", 0),
    ("probs", 1),
    ("expr", 0),
    ("grad", 4),
    ("add_near", 1),
    ("probs", 2),
    ("terms",),
    ("backward", 3),
    ("probs", 3),
    ("add_near", 2),
    ("backward", 4),
    ("add_far", 1),
    ("probs", 4),
    ("exchange",),
    ("add_near", 3),
    ("add_far", 2),
    ("left",),
    ("return",),
    ("loss",),
    ("add_far", 3),
    ("expr", 1),
    ("add_near", 4),
    ("logits",),
    ("add_far", 4),
    ("expr", 2),
    ("expr", 3),
    ("expr", 4),
)


def halves(value):
    high = value.astype(BF16)
    return high, (value - high.astype(F32)).astype(BF16)


def threefold(value):
    high, low = halves(value)
    return jnp.concatenate([high, high, low], axis=1)


def product(a, b, contract):
    return lax.dot_general(a, b, (contract, ((), ())), preferred_element_type=F32)


def plane_kernel(lines, forward_widths, backward_widths, *refs):
    chunks, turns = len(forward_widths), len(backward_widths)
    (
        (logits_ref, expr_ref, spatial_ref, count_in, cells_in, prior_in),
        (pr, loss_ref, glog, ge),
        (count_ref, cells_ref, prior_ref, lg, lq, tg, ex, pq, ab, af, probs_3, turned_3, expr_3, sacc, s1, s2, gv, ss, rowv, rs),
        (grad_3, factor, t0, p0, vr, fs, fx, fy, fz, fr, inn, l1, l2),
        (loc, ou_s, ou_r, od_s, od_r, fu_s, fu_r, fd_s, fd_r, a_s, a_r, a2_s, a2_r, r_s, r_r),
        (c_s, c_r, s1_s, s1_r, s2_s, s2_r, ss_s, ss_r, d_s, d_r, ru_s, ru_r, rd_s, rd_r),
        (f_s, f_r, fx_s, fx_r, go_s, go_r, in_s, in_r, l1_s, l1_r, l2_s, l2_r, t0_s, t0_r, p0_s, p0_r, vr_s, vr_r),
        bb,
        cs,
        cr,
        ds,
        es,
        ru,
        rd,
    ) = grouped(refs, (6, 4, 20, 13, 15, 14, 18, chunks, chunks, chunks, turns, turns, turns, turns))
    place = lax.axis_index("spot")
    core = lax.axis_index("gene")
    z = place // PLANE
    q = place % PLANE
    col, row = q % 2, q // 2
    mates = ((1 - row) * 2 + 1 - col, row * 2 + 1 - col, (1 - row) * 2 + col)
    others = tuple((z + step) % lines for step in range(1, lines))
    up, down = (place + PLANE, core), (place - PLANE, core)
    sibling = (place, 1 - core)
    slides, slide_rows = logits_ref.shape[0], logits_ref.shape[1]
    rows = slides * slide_rows
    cb = expr_ref.shape[0]
    genes = expr_ref.shape[1]
    last = lines - 1

    def mate(p):
        return (z * PLANE + p, core)

    def send(src, dst, send_sem, recv_sem, device):
        copy = pltpu.make_async_remote_copy(
            src_ref=src, dst_ref=dst, send_sem=send_sem, recv_sem=recv_sem, device_id=device, device_id_type=MESH
        )
        copy.start()

    def arrived(dst, recv_sem):
        pltpu.make_async_copy(dst, dst, recv_sem).wait()

    sent = arrived

    def cols(k):
        return pl.ds(sum(forward_widths[:k]), forward_widths[k])

    def turn_cols(k):
        return pl.ds(sum(backward_widths[:k]), backward_widths[k])

    def block(index):
        return pl.ds(pl.multiple_of(index * cb, cb), cb)

    def share(index):
        return pl.ds(pl.multiple_of(index * rows, rows), rows)

    def half(index):
        return pl.ds(pl.multiple_of(index * slide_rows, slide_rows), slide_rows)

    small = ((prior_in, prior_ref), (count_in, count_ref), (cells_in, cells_ref))
    pltpu.make_async_copy(expr_ref, ex, loc.at[2 * slides]).start()
    for m in range(slides):
        pltpu.make_async_copy(logits_ref.at[m], lg.at[half(m)], loc.at[m]).start()
    for at, (src, dst) in enumerate(small):
        pltpu.make_async_copy(src, dst, loc.at[2 * slides + 1 + at]).start()
    for m in range(slides):
        pltpu.make_async_copy(spatial_ref.at[m], tg.at[half(m)], loc.at[slides + m]).start()

    barrier = pltpu.get_barrier_semaphore()
    for p in mates:
        pl.semaphore_signal(barrier, inc=1, device_id=mate(p), device_id_type=MESH)
    for o in others:
        pl.semaphore_signal(barrier, inc=1, device_id=(o * PLANE + q, core), device_id_type=MESH)
    pl.semaphore_signal(barrier, inc=1, device_id=sibling, device_id_type=MESH)
    pltpu.make_async_copy(expr_ref, ex, loc.at[2 * slides]).wait()
    for k in range(chunks):
        bb[k][block(z), :] = ex[:, cols(k)]
    for m in range(slides):
        pltpu.make_async_copy(logits_ref.at[m], lg.at[half(m)], loc.at[m]).wait()
    for p in range(PLANE):
        for line in range(lines):
            lq[p, :, pl.ds(line * cb, cb)] = lg[half(core), pl.ds((line * PLANE + p) * cb, cb)]
    pl.semaphore_wait(barrier, len(mates) + len(others) + 1)

    def own_up(k):
        here = bb[k].at[block(z)]
        send(here, here, ou_s.at[k], ou_r.at[k], up)

    def own_down(k):
        here = bb[k].at[block(z)]
        send(here, here, od_s.at[k], od_r.at[k], down)

    def low(at):
        return 2 * at < lines

    for at in range(lines):

        @pl.when(z == at)
        def _():
            for k in range(chunks):
                if at < last and (at == 0 or k < (LEAD if low(at) else NEAR_LEAD)):
                    own_up(k)
                if at > 0 and (at == last or k < (NEAR_LEAD if low(at) else LEAD)):
                    own_down(k)

    for p in mates:
        send(lq.at[p], ab.at[q, half(core)], a_s, a_r.at[q], mate(p))

    def from_below(k, at):
        arrived(bb[k].at[pl.ds((at - 1) * cb, cb)], ou_r.at[k])
        if at > 1:
            arrived(bb[k].at[pl.ds(0, (at - 1) * cb)], fu_r.at[k])

    def from_above(k, at):
        arrived(bb[k].at[pl.ds((at + 1) * cb, cb)], od_r.at[k])
        if at < last - 1:
            arrived(bb[k].at[pl.ds((at + 2) * cb, (last - 1 - at) * cb)], fd_r.at[k])

    def upward(k, at):
        from_below(k, at)
        here = bb[k].at[pl.ds(0, at * cb)]
        send(here, here, fu_s.at[k], fu_r.at[k], up)

    def downward(k, at):
        from_above(k, at)
        here = bb[k].at[pl.ds((at + 1) * cb, (last - at) * cb)]
        send(here, here, fd_s.at[k], fd_r.at[k], down)

    def forward_far(k):
        for at in range(1, last):

            @pl.when(z == at)
            def _():
                (upward if low(at) else downward)(k, at)
                if k + LEAD < chunks:
                    (own_up if low(at) else own_down)(k + LEAD)

    def forward_near(k):
        for at in range(1, last):

            @pl.when(z == at)
            def _():
                (downward if low(at) else upward)(k, at)
                if k + NEAR_LEAD < chunks:
                    (own_down if low(at) else own_up)(k + NEAR_LEAD)

    def gathered(k):
        @pl.when(z == 0)
        def _():
            from_above(k, 0)

        @pl.when(z == last)
        def _():
            from_below(k, last)

    for at, (src, dst) in enumerate(small):
        pltpu.make_async_copy(src, dst, loc.at[2 * slides + 1 + at]).wait()
    weights = prior_ref[...].astype(F32) / fixed_point

    @pl.loop(0, rows // STEP_ROWS)
    def _(step):
        at = pl.ds(pl.multiple_of(step * STEP_ROWS, STEP_ROWS), STEP_ROWS)
        value = lg[at, :]
        peak = jnp.max(value, axis=1, keepdims=True)
        raised = jnp.exp(value - peak)
        scale = 1.0 / jnp.sum(raised, axis=1, keepdims=True)
        probs = raised * scale
        mass_rows = jnp.sum(probs * weights, axis=1, keepdims=True)
        rowv[0, at, :] = jnp.broadcast_to(mass_rows, (STEP_ROWS, LANES))
        rowv[1, at, :] = jnp.broadcast_to(peak, (STEP_ROWS, LANES))
        rowv[2, at, :] = jnp.broadcast_to(scale, (STEP_ROWS, LANES))
        for p in range(PLANE):
            for line in range(lines):
                at_cells = (line * PLANE + p) * cb
                pq[p, at, pl.ds(line * cb, cb)] = probs[:, at_cells : at_cells + cb]

    wide = lax.broadcasted_iota(jnp.int32, (rows, LANES), 1)
    rs[q] = jnp.where(wide == 0, rowv[1], rowv[2]).T[0:8]
    for p in mates:
        send(rs.at[q], rs.at[q], r_s, r_r.at[q], mate(p))

    rid = lax.broadcasted_iota(jnp.int32, (rows, 1), 0)
    first = rid < slide_rows
    position = place * slide_rows + jnp.where(first, rid, rid - slide_rows)
    count = jnp.where(first, count_ref[0], count_ref[1])
    valid = (position < count).astype(F32)
    scale_count = count.astype(F32)
    square = (slide_rows, slide_rows)
    eye = lax.broadcasted_iota(jnp.int32, square, 0) == lax.broadcasted_iota(jnp.int32, square, 1)
    counted = jnp.concatenate(
        [
            jnp.sum(jnp.where(eye, cells_ref[m : m + 1, :].astype(F32), 0.0), axis=1, keepdims=True)
            for m in range(slides)
        ],
        axis=0,
    )
    mass = rowv[0, :, 0:1]
    kcell = valid * counted

    def by_slide(value):
        return [jnp.sum(value[m * slide_rows : (m + 1) * slide_rows], axis=0, keepdims=True) for m in range(slides)]

    mass_parts = by_slide(valid * mass)
    cell_parts = by_slide(kcell)
    lane = lax.broadcasted_iota(jnp.int32, (1, LANES), 1)
    scalars = jnp.zeros((1, LANES), F32)
    for at, value in enumerate(mass_parts + cell_parts):
        scalars = jnp.where(lane == at, value, scalars)
    for m in range(slides):
        pltpu.make_async_copy(spatial_ref.at[m], tg.at[half(m)], loc.at[slides + m]).wait()

    head = backward_widths[0]
    t0[q] = tg[:, 0:head]
    for p in mates:
        send(t0.at[q], t0.at[q], t0_s, t0_r.at[q], mate(p))
    sacc[...] = jnp.zeros_like(sacc)
    s1[q, 3 * slides :, :] = jnp.zeros((8 - 3 * slides, genes), F32)
    s1[q, 3 * slides : 3 * slides + 1, 0:LANES] = scalars

    def share_logits():
        for p in (mates[1], mates[2], mates[0]):
            here = ab.at[p, half(core)]
            arrived(here, a_r.at[p])
            send(here, here, a2_s, a2_r.at[p], sibling)

    def lay_probs(p, at, value):
        af[p, at, :] = value
        there = pl.ds(pl.multiple_of(p * rows + at.start, BLOCK), BLOCK)
        probs_3[there, :] = threefold(value)

    def take_probs():
        in_blocks(0, rows, lambda at: lay_probs(q, at, pq[q, at, :]))
        for p in (mates[1], mates[2], mates[0]):
            arrived(rs.at[p], r_r.at[p])
            arrived(ab.at[p, half(1 - core)], a2_r.at[p])
            rowv[1] = jnp.concatenate([rs[p].T, jnp.zeros((rows, LANES - 8), F32)], axis=1)

            def take(at):
                probs = jnp.exp(ab[p, at, :] - rowv[1, at, 0:1]) * rowv[1, at, 1:2]
                lay_probs(p, at, probs)

            in_blocks(0, rows, take)

    def transpose(part):
        @pl.loop(0, PLANE // 2)
        def _(step):
            p = part * (PLANE // 2) + step
            high, low_part = halves(af[p].T)
            for third, value in enumerate((high, high, low_part)):
                turned_3[:, pl.ds(pl.multiple_of(third * PLANE * rows + p * rows, rows), rows)] = value

    def in_blocks(start, count, body):
        @pl.loop(0, count // BLOCK)
        def _(step):
            body(pl.ds(pl.multiple_of(start + step * BLOCK, BLOCK), BLOCK))

    quarter = lines * cb

    def lay_factor(at, length, width, value):
        high, low_part = halves(value)
        for third, part in enumerate((high, low_part, high)):
            here = pl.ds(pl.multiple_of(third * length + at.start, BLOCK), BLOCK)
            factor[here, 0:width] = part

    def keep_expr(k, at, value):
        start = sum(forward_widths[:k])
        for turn in range(turns):
            origin, width = sum(backward_widths[:turn]), backward_widths[turn]
            lo, hi = max(start, origin), min(start + forward_widths[k], origin + width)
            if lo < hi:
                high, low_part = halves(value[:, lo - start : hi - start])
                for third, part in enumerate((high, low_part, high)):
                    expr_3[at, pl.ds(3 * origin + third * width + lo - origin, hi - lo)] = part

    def three_turn_cols(k):
        return pl.ds(3 * sum(backward_widths[:k]), 3 * backward_widths[k])

    def forward_product(k):
        width = forward_widths[k]

        def lay(at):
            value = bb[k][at, :]
            lay_factor(at, quarter, width, value)
            keep_expr(k, at, value)

        in_blocks(0, quarter, lay)
        if k < chunks - 1:

            @pl.loop(0, PLANE * rows // TALL)
            def _(step):
                tall = pl.ds(pl.multiple_of(step * TALL, TALL), TALL)
                cs[k][tall, :] = product(probs_3[tall, :], factor[0 : 3 * quarter, 0:width], ((1,), (0,)))

            for p in mates:
                pass_pred(k, p)
        else:
            for side, served in ((1 - row, (mates[0], mates[2])), (row, (mates[1],))):
                pair = pl.ds(pl.multiple_of(2 * side * rows, 2 * rows), 2 * rows)
                cs[k][pair, :] = product(probs_3[pair, :], factor[0 : 3 * quarter, 0:width], ((1,), (0,)))
                for p in served:
                    pass_pred(k, p)

    def pass_pred(k, p):
        send(cs[k].at[share(p)], cr[k].at[q], c_s.at[k], c_r.at[k, q], mate(p))

    def finish_pred(k):
        total = cs[k][share(q), :]
        for p in mates:
            arrived(cr[k].at[p], c_r.at[k, p])
            total = total + cr[k][p]
        pr[:, cols(k)] = total
        if k == 0:
            p0[q] = total[:, 0:head]
            for p in mates:
                send(p0.at[q], p0.at[q], p0_s, p0_r.at[q], mate(p))
        truth = tg[:, cols(k)]
        for at, value in enumerate((total * truth, total * total, truth * truth)):
            sacc[at] += lane_groups(value)
        kept = valid * total
        stats = by_slide(kept * truth) + by_slide(kept * total) + by_slide(valid * truth * truth)
        s1[q, 0 : 3 * slides, cols(k)] = jnp.concatenate(stats, axis=0)

    early = sum(forward_widths[:EARLY])
    parts = (pl.ds(0, early), pl.ds(early, genes - early))

    def sum_plane(at):
        for p in mates:
            send(s1.at[q, :, parts[at]], s1.at[q, :, parts[at]], s1_s, s1_r.at[at, q], mate(p))

    def sum_line(at):
        for p in mates:
            arrived(s1.at[p, :, parts[at]], s1_r.at[at, p])
        s2[z, :, parts[at]] = (s1[0, :, parts[at]] + s1[1, :, parts[at]]) + (s1[2, :, parts[at]] + s1[3, :, parts[at]])
        for o in others:
            send(s2.at[z, :, parts[at]], s2.at[z, :, parts[at]], s2_s, s2_r.at[at, z], (o * PLANE + q, core))

    kept = {}

    def finish_genes(at):
        for o in others:
            arrived(s2.at[o, :, parts[at]], s2_r.at[at, o])
        total = s2[0, :, parts[at]]
        for line in range(1, lines):
            total = total + s2[line, :, parts[at]]
        gene_dot, gene_pred, gene_true = total[0:2], total[2:4], total[4:6]
        gene_inv = lax.rsqrt(gene_pred * gene_true + tiny)
        cos_gene = gene_dot * gene_inv
        gv[0:2, parts[at]] = gene_inv
        gv[2:4, parts[at]] = cos_gene * gene_true / (gene_pred * gene_true + tiny)
        kept["genes", at] = jnp.sum(jnp.sum(cos_gene, axis=1, keepdims=True), axis=0, keepdims=True)
        if at == 0:
            kept["mass"] = jnp.where(first, total[6:7, 0:1], total[6:7, 1:2])
            kept["cells"] = jnp.where(first, total[6:7, 2:3], total[6:7, 3:4])

    def sum_cores():
        sums = [jnp.sum(sacc[at], axis=1, keepdims=True) for at in range(3)]
        ss[core] = jnp.where(wide == 0, sums[0], jnp.where(wide == 1, sums[1], sums[2])).T[0:8]
        send(ss.at[core], ss.at[core], ss_s, ss_r, sibling)

    def finish_spots():
        lane_id = lax.broadcasted_iota(jnp.int32, (1, rows), 1)
        first_lane = lane_id < slide_rows
        lane_position = place * slide_rows + jnp.where(first_lane, lane_id, lane_id - slide_rows)
        lane_valid = (lane_position < jnp.where(first_lane, count_ref[0], count_ref[1])).astype(F32)
        arrived(ss.at[1 - core], ss_r)
        spot = ss[0] + ss[1]
        spot_dot, spot_pred, spot_true = spot[0:1], spot[1:2], spot[2:3]
        spot_inv = lax.rsqrt(spot_pred * spot_true + tiny)
        cos_spot = spot_dot * spot_inv
        spot_back = cos_spot * spot_true / (spot_pred * spot_true + tiny)
        kept["cos"] = jnp.sum(lane_valid * cos_spot, axis=1, keepdims=True)
        vectors = [lane_valid * spot_inv, lane_valid * spot_back, lane_valid, jnp.zeros((5, rows), F32)]
        vr[q] = jnp.concatenate(vectors, axis=0)
        sacc[0] = jnp.zeros_like(sacc[0])

    def gradient(truth, guess, by_row, k):
        pieces = []
        for m in range(slides):
            lo, hi = m * slide_rows, (m + 1) * slide_rows
            inverse, back = gv[m : m + 1, turn_cols(k)], gv[2 + m : 3 + m, turn_cols(k)]
            spot_inv, spot_back, spot_valid = by_row[lo:hi, 0:1], by_row[lo:hi, 1:2], by_row[lo:hi, 2:3]
            pieces.append(
                guess[lo:hi] * (spot_valid * back + spot_back) - truth[lo:hi] * (spot_valid * inverse + spot_inv)
            )
        return jnp.concatenate(pieces, axis=0)

    def head_gradient():
        for p in mates:
            arrived(t0.at[p], t0_r.at[p])
            arrived(p0.at[p], p0_r.at[p])
            arrived(vr.at[p], vr_r.at[p])
        for p in range(PLANE):
            ds[0][share(p), :] = gradient(t0[p], p0[p], vr[p].T, 0)
        sacc[0] += lane_groups(ds[0][share(q), :] * p0[q])

    def send_grad(k):
        if k == 0:
            for p in mates:
                send(vr.at[q], vr.at[q], vr_s, vr_r.at[q], mate(p))
            kept["by_row"] = vr[q].T
            return
        grad = gradient(tg[:, turn_cols(k)], pr[:, turn_cols(k)], kept["by_row"], k)
        here = ds[k].at[share(q)]
        here[...] = grad
        for p in mates:
            send(here, here, d_s.at[k], d_r.at[k, q], mate(p))
        sacc[0] += lane_groups(grad * pr[:, turn_cols(k)])

    def send_terms():
        mass_total, cell_total = kept["mass"], kept["cells"]
        portion = kcell / cell_total
        kl_rows = portion * (jnp.log(counted) - jnp.log(cell_total) - jnp.log(mass) + jnp.log(mass_total))
        dmass = scale_count * valid * (1.0 / mass_total - portion / mass)
        terms = jnp.sum(scale_count * kl_rows, axis=0, keepdims=True) - kept["cos"]
        l1[q] = jnp.broadcast_to(terms, (8, LANES))
        for p in mates:
            send(l1.at[q], l1.at[q], l1_s, l1_r.at[q], mate(p))
        inner = jnp.sum(sacc[0], axis=1, keepdims=True)
        inn[core] = jnp.where(wide == 0, inner, kept["genes", 0] + kept["genes", 1])
        send(inn.at[core], inn.at[core], in_s, in_r, sibling)
        rowv[1] = jnp.broadcast_to(dmass, (rows, LANES))

    middle = lines // 2

    def backward_product(k):
        if k == 0:
            head_gradient()
        else:
            for p in mates:
                arrived(ds[k].at[share(p)], d_r.at[k, p])
        width, spots = backward_widths[k], PLANE * rows

        def lay(at):
            value = ds[k][at, :]
            lay_factor(at, spots, width, value)
            grad_3[at, three_turn_cols(k)] = threefold(value)

        in_blocks(0, spots, lay)
        if not halved(k):

            @pl.loop(0, quarter // TALL)
            def _(step):
                tall = pl.ds(pl.multiple_of(step * TALL, TALL), TALL)
                es[k][tall, :] = product(turned_3[tall, :], factor[0 : 3 * spots, 0:width], ((1,), (0,)))

        for turn in range(2):
            if halved(k):
                side = (1 - z // middle) if turn == 0 else z // middle
                pair = pl.ds(pl.multiple_of(side * middle * cb, middle * cb), middle * cb)
                es[k][pair, :] = product(turned_3[pair, :], factor[0 : 3 * spots, 0:width], ((1,), (0,)))

            @pl.when(z == 0)
            def _():
                if halved(k):
                    pass_up(k, middle if turn == 0 else 1, middle if turn == 0 else middle - 1, turn)
                elif whole(k):
                    if turn == 0:
                        pass_up(k, 1, last, 0)
                elif turn == 0:
                    for line in range(last, 0, -1):
                        pass_up(k, line, 1, line)

            @pl.when(z == last)
            def _():
                if halved(k):
                    pass_down(k, 0 if turn == 0 else middle, middle if turn == 0 else middle - 1, turn)
                elif whole(k):
                    if turn == 0:
                        pass_down(k, 0, last, 0)
                elif turn == 0:
                    for line in range(last):
                        pass_down(k, line, 1, line)

    def halved(k):
        return k == 0

    def whole(k):
        return 0 < k < turns - SPLIT

    def pass_up(k, line, count, slot):
        here = pl.ds(line * cb, count * cb)
        send(es[k].at[here], ru[k].at[here], ru_s.at[k], ru_r.at[k, slot], up)

    def pass_down(k, line, count, slot):
        here = pl.ds(line * cb, count * cb)
        send(es[k].at[here], rd[k].at[here], rd_s.at[k], rd_r.at[k, slot], down)

    def take_up(k, line, count, slot):
        arrived(ru[k].at[pl.ds(line * cb, count * cb)], ru_r.at[k, slot])

    def take_down(k, line, count, slot):
        arrived(rd[k].at[pl.ds(line * cb, count * cb)], rd_r.at[k, slot])

    def add_up(k, line, count):
        def add(at):
            es[k][at, :] += ru[k][at, :]

        in_blocks(line * cb, count * cb, add)

    def add_down(k, line, count):
        def add(at):
            es[k][at, :] += rd[k][at, :]

        in_blocks(line * cb, count * cb, add)

    def rising(k, at):
        if halved(k) or whole(k):
            start = middle if halved(k) else at
            take_up(k, start, lines - start, 0)
            above = max(at + 1, start)
            add_up(k, above, lines - above)
            pass_up(k, above, lines - above, 0)
        else:
            for line in range(last, at, -1):
                take_up(k, line, 1, line)
                add_up(k, line, 1)
                pass_up(k, line, 1, line)

    def falling(k, at):
        if halved(k) or whole(k):
            end = middle if halved(k) else at + 1
            take_down(k, 0, end, 0)
            below = min(at, end)
            add_down(k, 0, below)
            pass_down(k, 0, below, 0)
        else:
            for line in range(at):
                take_down(k, line, 1, line)
                add_down(k, line, 1)
                pass_down(k, line, 1, line)

    def add_near(k):
        for at in range(1, last):

            @pl.when(z == at)
            def _():
                (rising if low(at) else falling)(k, at)

    def add_far(k):
        for at in range(1, last):

            @pl.when(z == at)
            def _():
                (falling if low(at) else rising)(k, at)

    def finish_expr(k):
        for at in range(lines):

            @pl.when(z == at)
            def _():
                if at > 0:
                    if halved(k) and at < middle:
                        take_up(k, at, 1, 1)
                    elif at == last and (halved(k) or whole(k)):
                        take_up(k, at, 1, 0)
                    elif not halved(k) and not whole(k):
                        take_up(k, at, 1, at)
                if at < last:
                    if halved(k) and at >= middle:
                        take_down(k, at, 1, 1)
                    elif at == 0 and (halved(k) or whole(k)):
                        take_down(k, at, 1, 0)
                    elif not halved(k) and not whole(k):
                        take_down(k, at, 1, at)

        from_low, from_high = z > 0, z < last

        @pl.loop(0, cb // BLOCK)
        def _(step):
            here = pl.ds(pl.multiple_of(step * BLOCK, BLOCK), BLOCK)
            own = pl.ds(pl.multiple_of(z * cb + step * BLOCK, BLOCK), BLOCK)
            total = es[k][own, :]
            total = total + jnp.where(from_low, ru[k][own, :], 0.0)
            ge[here, turn_cols(k)] = total + jnp.where(from_high, rd[k][own, :], 0.0)

    def probs_gradient(k):
        at = three_turn_cols(k)

        @pl.loop(0, PLANE * rows // TALL)
        def _(step):
            tall = pl.ds(pl.multiple_of(step * TALL, TALL), TALL)
            part = product(grad_3[tall, at], expr_3[:, at], ((1,), (1,)))
            if k == 0:
                fs[tall, :] = part
            else:
                fs[tall, :] += part

    def slide_of(p, m):
        return pl.ds(pl.multiple_of(p * rows + m * slide_rows, slide_rows), slide_rows)

    def sum_probs_cores():
        for p in mates + (q,):
            fx[p] = fs[slide_of(p, 1 - core), :]
            send(fx.at[p], fy.at[p], fx_s, fx_r.at[p], sibling)

    def return_probs():
        for p in mates:
            arrived(fy.at[p], fx_r.at[p])
            fz[p] = fs[slide_of(p, core), :] + fy[p]
            send(fz.at[p], fr.at[q], f_s, f_r.at[q], mate(p))
        arrived(fy.at[q], fx_r.at[q])
        fr[q] = fs[slide_of(q, core), :] + fy[q]

    def pass_terms():
        for p in mates:
            arrived(l1.at[p], l1_r.at[p])
        l2[z] = (l1[0] + l1[1]) + (l1[2] + l1[3])
        for o in others:
            send(l2.at[z], l2.at[z], l2_s, l2_r.at[z], (o * PLANE + q, core))

    def part_of(slide, m):
        start = slide * slide_rows + m * (slide_rows // 2)
        return pl.ds(pl.multiple_of(start, slide_rows // 2), slide_rows // 2)

    def finish_logits():
        arrived(inn.at[1 - core], in_r)
        rowv[2] = (inn[0] + inn[1]) + rowv[1] * rowv[0]
        for p in mates:
            arrived(fr.at[p], f_r.at[p])
        for m in range(2):

            @pl.loop(0, slide_rows // STEP_ROWS // 2)
            def _(step):
                row_at = (m * (slide_rows // STEP_ROWS // 2) + step) * STEP_ROWS
                at = pl.ds(pl.multiple_of(row_at, STEP_ROWS), STEP_ROWS)
                whole_at = pl.ds(pl.multiple_of(core * slide_rows + row_at, STEP_ROWS), STEP_ROWS)
                by_mass, total_inner = rowv[1, whole_at, 0:1], rowv[2, whole_at, 0:1]
                for p in range(PLANE):
                    for line in range(lines):
                        here, there = pl.ds(line * cb, cb), (line * PLANE + p) * cb
                        grad = fr[p, at, here] + by_mass * weights[:, there : there + cb]
                        glog[whole_at, pl.ds(there, cb)] = pq[p, whole_at, here] * (grad - total_inner)

            here = part_of(core, m)
            send(glog.at[here], glog.at[here], go_s, go_r.at[m], sibling)

    def forward_left():
        for k in range(chunks):

            @pl.when(z < last)
            def _():
                sent(bb[k].at[block(z)], ou_s.at[k])

            @pl.when(z > 0)
            def _():
                sent(bb[k].at[block(z)], od_s.at[k])

            for at in range(1, last):

                @pl.when(z == at)
                def _():
                    sent(bb[k].at[pl.ds(0, at * cb)], fu_s.at[k])
                    sent(bb[k].at[pl.ds((at + 1) * cb, (last - at) * cb)], fd_s.at[k])

        three = pl.ds(0, len(mates))
        sent(ab.at[three, half(0)], a_s)
        sent(ab.at[three, half(0)], a2_s)
        sent(rs.at[three], r_s)
        sent(t0.at[three], t0_s)
        sent(p0.at[three], p0_s)
        for k in range(chunks):
            sent(cr[k].at[three], c_s.at[k])
        sent(s1.at[three], s1_s)
        sent(s2.at[pl.ds(0, last)], s2_s)
        sent(ss.at[0], ss_s)

    steps = {
        "far": forward_far,
        "near": forward_near,
        "share": share_logits,
        "take": take_probs,
        "whole": gathered,
        "product": forward_product,
        "sum": finish_pred,
        "turn": transpose,
        "plane": sum_plane,
        "line": sum_line,
        "genes": finish_genes,
        "cores": sum_cores,
        "spots": finish_spots,
        "grad": send_grad,
        "terms": send_terms,
        "backward": backward_product,
        "probs": probs_gradient,
        "exchange": sum_probs_cores,
        "return": return_probs,
        "loss": pass_terms,
        "logits": finish_logits,
        "add_near": add_near,
        "add_far": add_far,
        "expr": finish_expr,
        "left": forward_left,
    }
    for name, *where in STEPS:
        steps[name](*where)

    for o in others:
        arrived(l2.at[o], l2_r.at[o])
    loss = l2[0]
    for line in range(1, lines):
        loss = loss + l2[line]
    loss_ref[...] = loss[0:1, 0:1] - (inn[0, 0:1, 1:2] + inn[1, 0:1, 1:2])
    for m in range(2):
        arrived(glog.at[part_of(1 - core, m)], go_r.at[m])

    for k in range(turns):
        for at in range(lines):

            @pl.when(z == at)
            def _():
                if at < last:
                    sent(es[k].at[pl.ds((at + 1) * cb, (last - at) * cb)], ru_s.at[k])
                if at > 0:
                    sent(es[k].at[pl.ds(0, at * cb)], rd_s.at[k])

    three = pl.ds(0, len(mates))
    for k in range(1, turns):
        sent(ds[k].at[pl.ds(0, len(mates) * rows)], d_s.at[k])
    sent(vr.at[three], vr_s)
    sent(inn.at[0], in_s)
    sent(l1.at[three], l1_s)
    sent(l2.at[pl.ds(0, last)], l2_s)
    sent(fr.at[three], f_s)
    sent(fx, fx_s)
    sent(glog.at[half(0)], go_s)


def lane_groups(value):
    parts = [value[:, at : at + LANES] for at in range(0, value.shape[1], LANES)]
    return functools.reduce(lambda a, b: a + b, parts)


def grouped(refs, sizes):
    at = 0
    for size in sizes:
        yield refs[at : at + size]
        at += size


def deliver(pred_in, loss_in, glog_in, gexp_in, pred_ref, loss_ref, glog_ref, gexp_ref, sems):
    slides, slide_rows = pred_ref.shape[0], pred_ref.shape[1]
    pairs = [(gexp_in, gexp_ref), (loss_in, loss_ref)]
    for m in range(slides):
        part = pl.ds(m * slide_rows, slide_rows)
        pairs += [(glog_in.at[part], glog_ref.at[m]), (pred_in.at[part], pred_ref.at[m])]
    copies = [pltpu.make_async_copy(src, dst, sems.at[at]) for at, (src, dst) in enumerate(pairs)]
    for copy in copies:
        copy.start()
    for copy in copies:
        copy.wait()


def plane_call(logits, expr, spatial, slide_spots, spot_cells, cell_prior, lines):
    slides, slide_rows, cells = logits.shape
    rows = slides * slide_rows
    cb, genes = expr.shape
    quarter = lines * cb
    spots = PLANE * rows
    chunks, turns = len(FORWARD), len(BACKWARD)
    dma = pltpu.SemaphoreType.DMA
    vmem = pltpu.VMEM
    anywhere = pl.BlockSpec(memory_space=pl.ANY)
    in_vmem = pl.BlockSpec(memory_space=pltpu.VMEM)
    scratch = [
        pltpu.SMEM((slides,), jnp.int32),
        vmem((slides, slide_rows), jnp.int32),
        vmem((1, cells), jnp.int32),
        vmem((rows, cells), F32),
        vmem((PLANE, slide_rows, quarter), F32),
        vmem((rows, genes), F32),
        vmem((cb, genes), F32),
        vmem((PLANE, rows, quarter), F32),
        vmem((PLANE, rows, quarter), F32),
        vmem((PLANE, rows, quarter), F32),
        vmem((spots, 3 * quarter), BF16),
        vmem((quarter, 3 * spots), BF16),
        vmem((quarter, 3 * genes), BF16),
        vmem((3, rows, LANES), F32),
        vmem((PLANE, 8, genes), F32),
        vmem((lines, 8, genes), F32),
        vmem((8, genes), F32),
        vmem((2, 8, rows), F32),
        vmem((3, rows, LANES), F32),
        vmem((PLANE, 8, rows), F32),
        vmem((spots, 3 * genes), BF16),
        vmem((3 * max(quarter, spots), max(FORWARD + BACKWARD)), BF16),
        vmem((PLANE, rows, BACKWARD[0]), F32),
        vmem((PLANE, rows, BACKWARD[0]), F32),
        vmem((PLANE, 8, rows), F32),
        vmem((spots, quarter), F32),
        vmem((PLANE, slide_rows, quarter), F32),
        vmem((PLANE, slide_rows, quarter), F32),
        vmem((PLANE, slide_rows, quarter), F32),
        vmem((PLANE, slide_rows, quarter), F32),
        vmem((2, rows, LANES), F32),
        vmem((PLANE, 8, LANES), F32),
        vmem((lines, 8, LANES), F32),
        dma((2 * slides + 4,)),
        dma((chunks,)),
        dma((chunks,)),
        dma((chunks,)),
        dma((chunks,)),
        dma((chunks,)),
        dma((chunks,)),
        dma((chunks,)),
        dma((chunks,)),
        dma,
        dma((PLANE,)),
        dma,
        dma((PLANE,)),
        dma,
        dma((PLANE,)),
        dma((chunks,)),
        dma((chunks, PLANE)),
        dma,
        dma((2, PLANE)),
        dma,
        dma((2, lines)),
        dma,
        dma,
        dma((turns,)),
        dma((turns, PLANE)),
        dma((turns,)),
        dma((turns, lines)),
        dma((turns,)),
        dma((turns, lines)),
        dma,
        dma((PLANE,)),
        dma,
        dma((PLANE,)),
        dma,
        dma((2,)),
        dma,
        dma,
        dma,
        dma((PLANE,)),
        dma,
        dma((lines,)),
        dma,
        dma((PLANE,)),
        dma,
        dma((PLANE,)),
        dma,
        dma((PLANE,)),
    ]
    for shape, widths in (
        ((quarter,), FORWARD),
        ((spots,), FORWARD),
        ((PLANE, rows), FORWARD),
        ((spots,), BACKWARD),
        ((quarter,), BACKWARD),
        ((quarter,), BACKWARD),
        ((quarter,), BACKWARD),
    ):
        scratch += [vmem(shape + (width,), F32) for width in widths]
    in_hbm = functools.partial(pltpu.with_memory_space_constraint, memory_space=pltpu.HBM)
    in_place = functools.partial(pltpu.with_memory_space_constraint, memory_space=pltpu.VMEM)
    results = pl.pallas_call(
        functools.partial(plane_kernel, lines, FORWARD, BACKWARD),
        out_shape=(
            vmem((rows, genes), F32),
            vmem((1, 1), F32),
            vmem((rows, cells), F32),
            vmem((cb, genes), F32),
        ),
        in_specs=[anywhere] * 6,
        out_specs=(in_vmem,) * 4,
        scratch_shapes=scratch,
        compiler_params=pltpu.CompilerParams(
            collective_id=0, has_side_effects=True, vmem_limit_bytes=48 * 1024 * 1024
        ),
    )(*map(in_hbm, (logits, expr, spatial, slide_spots, spot_cells, cell_prior.reshape(1, cells))))
    pred, loss, grad_logits, grad_expr = pl.pallas_call(
        deliver,
        out_shape=(
            jax.ShapeDtypeStruct((slides, slide_rows, genes), F32),
            jax.ShapeDtypeStruct((1, 1), F32),
            jax.ShapeDtypeStruct((slides, slide_rows, cells), F32),
            jax.ShapeDtypeStruct((cb, genes), F32),
        ),
        in_specs=[anywhere] * 4,
        out_specs=(anywhere,) * 4,
        scratch_shapes=[dma((2 * slides + 2,))],
        compiler_params=pltpu.CompilerParams(vmem_limit_bytes=4 * 1024 * 1024),
    )(*map(in_place, results))
    return pred, loss.reshape(()), grad_logits, grad_expr


def general_plan(logits, expr, spatial, slide_spots, spot_cells, cell_prior):
    place = lax.axis_index("spot")
    side = lax.axis_index("gene")
    rows_all = logits.shape[1]
    cell_rows = expr.shape[0]
    weights = cell_prior.astype(jnp.float32) / fixed_point
    gene_share = (place == 0).astype(jnp.float32)
    row_share = (side == 0).astype(jnp.float32)
    own_weights = lax.dynamic_slice_in_dim(weights, place * cell_rows, cell_rows, 0)
    expr_acc = jnp.zeros((cell_rows, expr.shape[1]), jnp.float32)
    loss_local = jnp.zeros((), jnp.float32)
    pred_list = []
    grad_list = []
    for slide in range(logits.shape[0]):
        logit_rows = logits[slide]
        counted = spot_cells[slide].astype(jnp.float32)
        target = spatial[slide]
        positions = place * rows_all + jnp.arange(rows_all, dtype=jnp.int32)
        valid = (positions < slide_spots[slide]).astype(jnp.float32)
        peak = jnp.max(logit_rows, axis=1, keepdims=True)
        raised = jnp.exp(logit_rows - peak)
        probs = raised / jnp.sum(raised, axis=1, keepdims=True)
        mass = jnp.dot(probs, weights, precision=lax.Precision.HIGHEST)
        blocks = lax.all_to_all(probs, "spot", split_axis=1, concat_axis=0, tiled=True)
        pred = lax.psum_scatter(
            jnp.dot(blocks, expr, precision=lax.Precision.HIGHEST),
            "spot",
            scatter_dimension=0,
            tiled=True,
        )
        gene_dot = jnp.sum(valid[:, None] * pred * target, axis=0)
        gene_pred = jnp.sum(valid[:, None] * pred * pred, axis=0)
        gene_true = jnp.sum(valid[:, None] * target * target, axis=0)
        mass_part = jnp.sum(valid * mass)
        kcell = valid * counted
        cell_part = jnp.sum(kcell)
        spot_dot = jnp.sum(pred * target, axis=1)
        spot_pred = jnp.sum(pred * pred, axis=1)
        spot_true = jnp.sum(target * target, axis=1)
        gene_dot, gene_pred, gene_true, mass_total, cell_total = lax.psum(
            (gene_dot, gene_pred, gene_true, mass_part, cell_part), "spot"
        )
        spot_dot, spot_pred, spot_true = lax.psum((spot_dot, spot_pred, spot_true), "gene")
        gene_inv = lax.rsqrt(gene_pred * gene_true + tiny)
        cos_gene = gene_dot * gene_inv
        spot_inv = lax.rsqrt(spot_pred * spot_true + tiny)
        cos_spot = spot_dot * spot_inv
        share = kcell / cell_total
        scale_count = slide_spots[slide].astype(jnp.float32)
        kl_part = jnp.sum(
            share * (jnp.log(counted) - jnp.log(cell_total) - jnp.log(mass) + jnp.log(mass_total))
        )
        loss_local = loss_local - gene_share * jnp.sum(cos_gene)
        loss_local = loss_local + row_share * (scale_count * kl_part - jnp.sum(valid * cos_spot))
        gene_back = cos_gene * gene_true / (gene_pred * gene_true + tiny)
        spot_back = cos_spot * spot_true / (spot_pred * spot_true + tiny)
        dpred = -valid[:, None] * (
            target * (gene_inv[None, :] + spot_inv[:, None])
            - pred * gene_back[None, :]
            - pred * spot_back[:, None]
        )
        dmass = scale_count * valid * (1.0 / mass_total - share / mass)
        pred_list.append(pred)
        grads_full, mass_full = (
            lax.all_gather(dpred, "spot", axis=0, tiled=True),
            lax.all_gather(dmass, "spot", axis=0, tiled=True),
        )
        dprob_cells = jnp.dot(grads_full, expr.T, precision=lax.Precision.HIGHEST)
        dprob_cells = lax.psum(dprob_cells, "gene")
        expr_acc = expr_acc + lax.dot_general(
            blocks, grads_full, (((0,), (0,)), ((), ())), precision=lax.Precision.HIGHEST
        )
        dprob_cells = dprob_cells + mass_full[:, None] * own_weights[None, :]
        dprob_rows = lax.all_to_all(dprob_cells, "spot", split_axis=0, concat_axis=1, tiled=True)
        inner = jnp.sum(probs * dprob_rows, axis=1, keepdims=True)
        dlogit = probs * (dprob_rows - inner)
        grad_list.append(dlogit)
    loss = lax.psum(loss_local, ("spot", "gene"))
    return (jnp.stack(pred_list), loss, jnp.stack(grad_list), expr_acc)


def solution(mesh):
    places = mesh.shape["spot"]

    def on_device(logits, expr, spatial, slide_spots, spot_cells, cell_prior):
        if places == PLANE * PLANE and mesh.shape["gene"] == 2 and expr.shape[1] == sum(FORWARD):
            return plane_call(
                logits, expr, spatial, slide_spots, spot_cells, cell_prior, places // PLANE
            )
        return general_plan(logits, expr, spatial, slide_spots, spot_cells, cell_prior)

    in_specs = (
        P(None, "spot", None),
        P("spot", "gene"),
        P(None, "spot", "gene"),
        P(),
        P(None, "spot"),
        P(),
    )
    out_specs = (P(None, "spot", "gene"), P(), P(None, "spot", None), P("spot", "gene"))
    return jax.shard_map(
        on_device, mesh=mesh, in_specs=in_specs, out_specs=out_specs, check_vma=False
    )
```

```python
import functools

import jax
import jax.numpy as jnp
from jax import lax
from jax.experimental import pallas as pl
from jax.experimental.pallas import tpu as pltpu
from jax.sharding import PartitionSpec as P

tiny = 1e-06
fixed_point = 16384.0
F32 = jnp.float32
BF16 = jnp.bfloat16
MESH = pl.DeviceIdType.MESH

PLANE = 4
LANES = 128
STEP_ROWS = 16
BLOCK = 32
TALL = 256
FORWARD = (128, 256, 256, 256, 128)
BACKWARD = (128, 128, 256, 256, 256)
SPLIT = 4
LEAD = 1
NEAR_LEAD = 2
EARLY = 3
STEPS = (
    ("far", 0),
    ("far", 1),
    ("near", 0),
    ("share",),
    ("far", 2),
    ("far", 3),
    ("take",),
    ("whole", 0),
    ("near", 1),
    ("product", 0),
    ("sum", 0),
    ("whole", 1),
    ("near", 2),
    ("product", 1),
    ("whole", 2),
    ("product", 2),
    ("whole", 3),
    ("near", 3),
    ("product", 3),
    ("whole", 4),
    ("far", 4),
    ("near", 4),
    ("product", 4),
    ("turn", 0),
    ("sum", 1),
    ("sum", 2),
    ("plane", 0),
    ("turn", 1),
    ("sum", 3),
    ("line", 0),
    ("sum", 4),
    ("plane", 1),
    ("cores",),
    ("genes", 0),
    ("spots",),
    ("grad", 0),
    ("grad", 1),
    ("grad", 2),
    ("line", 1),
    ("backward", 0),
    ("backward", 1),
    ("add_near", 0),
    ("genes", 1),
    ("grad", 3),
    ("backward", 2),
    ("probs", 0),
    ("add_far", 0),
    ("probs", 1),
    ("expr", 0),
    ("grad", 4),
    ("add_near", 1),
    ("probs", 2),
    ("terms",),
    ("backward", 3),
    ("probs", 3),
    ("add_near", 2),
    ("backward", 4),
    ("add_far", 1),
    ("probs", 4),
    ("exchange",),
    ("add_near", 3),
    ("add_far", 2),
    ("left",),
    ("return",),
    ("loss",),
    ("add_far", 3),
    ("expr", 1),
    ("add_near", 4),
    ("logits",),
    ("add_far", 4),
    ("expr", 2),
    ("expr", 3),
    ("expr", 4),
)


def halves(value):
    high = value.astype(BF16)
    return high, (value - high.astype(F32)).astype(BF16)


def threefold(value):
    high, low = halves(value)
    return jnp.concatenate([high, high, low], axis=1)


def product(a, b, contract):
    return lax.dot_general(a, b, (contract, ((), ())), preferred_element_type=F32)


def plane_kernel(lines, forward_widths, backward_widths, *refs):
    chunks, turns = len(forward_widths), len(backward_widths)
    (
        (logits_ref, expr_ref, spatial_ref, count_in, cells_in, prior_in),
        (pr, loss_ref, glog, ge),
        (count_ref, cells_ref, prior_ref, lg, lq, tg, ex, pq, ab, af, probs_3, turned_3, expr_3, sacc, s1, s2, gv, ss, rowv, rs),
        (grad_3, factor, t0, p0, vr, fs, fx, fy, fz, fr, inn, l1, l2),
        (loc, ou_s, ou_r, od_s, od_r, fu_s, fu_r, fd_s, fd_r, a_s, a_r, a2_s, a2_r, r_s, r_r),
        (c_s, c_r, s1_s, s1_r, s2_s, s2_r, ss_s, ss_r, d_s, d_r, ru_s, ru_r, rd_s, rd_r),
        (f_s, f_r, fx_s, fx_r, go_s, go_r, in_s, in_r, l1_s, l1_r, l2_s, l2_r, t0_s, t0_r, p0_s, p0_r, vr_s, vr_r),
        bb,
        cs,
        cr,
        ds,
        es,
        ru,
        rd,
    ) = grouped(refs, (6, 4, 20, 13, 15, 14, 18, chunks, chunks, chunks, turns, turns, turns, turns))
    place = lax.axis_index("spot")
    core = lax.axis_index("gene")
    z = place // PLANE
    q = place % PLANE
    col, row = q % 2, q // 2
    mates = ((1 - row) * 2 + 1 - col, row * 2 + 1 - col, (1 - row) * 2 + col)
    others = tuple((z + step) % lines for step in range(1, lines))
    up, down = (place + PLANE, core), (place - PLANE, core)
    sibling = (place, 1 - core)
    slides, slide_rows = logits_ref.shape[0], logits_ref.shape[1]
    rows = slides * slide_rows
    cb = expr_ref.shape[0]
    genes = expr_ref.shape[1]
    last = lines - 1

    def mate(p):
        return (z * PLANE + p, core)

    def send(src, dst, send_sem, recv_sem, device):
        copy = pltpu.make_async_remote_copy(
            src_ref=src, dst_ref=dst, send_sem=send_sem, recv_sem=recv_sem, device_id=device, device_id_type=MESH
        )
        copy.start()

    def arrived(dst, recv_sem):
        pltpu.make_async_copy(dst, dst, recv_sem).wait()

    sent = arrived

    def cols(k):
        return pl.ds(sum(forward_widths[:k]), forward_widths[k])

    def turn_cols(k):
        return pl.ds(sum(backward_widths[:k]), backward_widths[k])

    def block(index):
        return pl.ds(pl.multiple_of(index * cb, cb), cb)

    def share(index):
        return pl.ds(pl.multiple_of(index * rows, rows), rows)

    def half(index):
        return pl.ds(pl.multiple_of(index * slide_rows, slide_rows), slide_rows)

    small = ((prior_in, prior_ref), (count_in, count_ref), (cells_in, cells_ref))
    pltpu.make_async_copy(expr_ref, ex, loc.at[2 * slides]).start()
    for m in range(slides):
        pltpu.make_async_copy(logits_ref.at[m], lg.at[half(m)], loc.at[m]).start()
    for at, (src, dst) in enumerate(small):
        pltpu.make_async_copy(src, dst, loc.at[2 * slides + 1 + at]).start()
    for m in range(slides):
        pltpu.make_async_copy(spatial_ref.at[m], tg.at[half(m)], loc.at[slides + m]).start()

    barrier = pltpu.get_barrier_semaphore()
    for p in mates:
        pl.semaphore_signal(barrier, inc=1, device_id=mate(p), device_id_type=MESH)
    for o in others:
        pl.semaphore_signal(barrier, inc=1, device_id=(o * PLANE + q, core), device_id_type=MESH)
    pl.semaphore_signal(barrier, inc=1, device_id=sibling, device_id_type=MESH)
    pltpu.make_async_copy(expr_ref, ex, loc.at[2 * slides]).wait()
    for k in range(chunks):
        bb[k][block(z), :] = ex[:, cols(k)]
    for m in range(slides):
        pltpu.make_async_copy(logits_ref.at[m], lg.at[half(m)], loc.at[m]).wait()
    for p in range(PLANE):
        for line in range(lines):
            lq[p, :, pl.ds(line * cb, cb)] = lg[half(core), pl.ds((line * PLANE + p) * cb, cb)]
    pl.semaphore_wait(barrier, len(mates) + len(others) + 1)

    def own_up(k):
        here = bb[k].at[block(z)]
        send(here, here, ou_s.at[k], ou_r.at[k], up)

    def own_down(k):
        here = bb[k].at[block(z)]
        send(here, here, od_s.at[k], od_r.at[k], down)

    def low(at):
        return 2 * at < lines

    for at in range(lines):

        @pl.when(z == at)
        def _():
            for k in range(chunks):
                if at < last and (at == 0 or k < (LEAD if low(at) else NEAR_LEAD)):
                    own_up(k)
                if at > 0 and (at == last or k < (NEAR_LEAD if low(at) else LEAD)):
                    own_down(k)

    for p in mates:
        send(lq.at[p], ab.at[q, half(core)], a_s, a_r.at[q], mate(p))

    def from_below(k, at):
        arrived(bb[k].at[pl.ds((at - 1) * cb, cb)], ou_r.at[k])
        if at > 1:
            arrived(bb[k].at[pl.ds(0, (at - 1) * cb)], fu_r.at[k])

    def from_above(k, at):
        arrived(bb[k].at[pl.ds((at + 1) * cb, cb)], od_r.at[k])
        if at < last - 1:
            arrived(bb[k].at[pl.ds((at + 2) * cb, (last - 1 - at) * cb)], fd_r.at[k])

    def upward(k, at):
        from_below(k, at)
        here = bb[k].at[pl.ds(0, at * cb)]
        send(here, here, fu_s.at[k], fu_r.at[k], up)

    def downward(k, at):
        from_above(k, at)
        here = bb[k].at[pl.ds((at + 1) * cb, (last - at) * cb)]
        send(here, here, fd_s.at[k], fd_r.at[k], down)

    def forward_far(k):
        for at in range(1, last):

            @pl.when(z == at)
            def _():
                (upward if low(at) else downward)(k, at)
                if k + LEAD < chunks:
                    (own_up if low(at) else own_down)(k + LEAD)

    def forward_near(k):
        for at in range(1, last):

            @pl.when(z == at)
            def _():
                (downward if low(at) else upward)(k, at)
                if k + NEAR_LEAD < chunks:
                    (own_down if low(at) else own_up)(k + NEAR_LEAD)

    def gathered(k):
        @pl.when(z == 0)
        def _():
            from_above(k, 0)

        @pl.when(z == last)
        def _():
            from_below(k, last)

    for at, (src, dst) in enumerate(small):
        pltpu.make_async_copy(src, dst, loc.at[2 * slides + 1 + at]).wait()
    weights = prior_ref[...].astype(F32) / fixed_point

    @pl.loop(0, rows // STEP_ROWS)
    def _(step):
        at = pl.ds(pl.multiple_of(step * STEP_ROWS, STEP_ROWS), STEP_ROWS)
        value = lg[at, :]
        peak = jnp.max(value, axis=1, keepdims=True)
        raised = jnp.exp(value - peak)
        scale = 1.0 / jnp.sum(raised, axis=1, keepdims=True)
        probs = raised * scale
        mass_rows = jnp.sum(probs * weights, axis=1, keepdims=True)
        rowv[0, at, :] = jnp.broadcast_to(mass_rows, (STEP_ROWS, LANES))
        rowv[1, at, :] = jnp.broadcast_to(peak, (STEP_ROWS, LANES))
        rowv[2, at, :] = jnp.broadcast_to(scale, (STEP_ROWS, LANES))
        for p in range(PLANE):
            for line in range(lines):
                at_cells = (line * PLANE + p) * cb
                pq[p, at, pl.ds(line * cb, cb)] = probs[:, at_cells : at_cells + cb]

    wide = lax.broadcasted_iota(jnp.int32, (rows, LANES), 1)
    rs[q] = jnp.where(wide == 0, rowv[1], rowv[2]).T[0:8]
    for p in mates:
        send(rs.at[q], rs.at[q], r_s, r_r.at[q], mate(p))

    rid = lax.broadcasted_iota(jnp.int32, (rows, 1), 0)
    first = rid < slide_rows
    position = place * slide_rows + jnp.where(first, rid, rid - slide_rows)
    count = jnp.where(first, count_ref[0], count_ref[1])
    valid = (position < count).astype(F32)
    scale_count = count.astype(F32)
    square = (slide_rows, slide_rows)
    eye = lax.broadcasted_iota(jnp.int32, square, 0) == lax.broadcasted_iota(jnp.int32, square, 1)
    counted = jnp.concatenate(
        [
            jnp.sum(jnp.where(eye, cells_ref[m : m + 1, :].astype(F32), 0.0), axis=1, keepdims=True)
            for m in range(slides)
        ],
        axis=0,
    )
    mass = rowv[0, :, 0:1]
    kcell = valid * counted

    def by_slide(value):
        return [jnp.sum(value[m * slide_rows : (m + 1) * slide_rows], axis=0, keepdims=True) for m in range(slides)]

    mass_parts = by_slide(valid * mass)
    cell_parts = by_slide(kcell)
    lane = lax.broadcasted_iota(jnp.int32, (1, LANES), 1)
    scalars = jnp.zeros((1, LANES), F32)
    for at, value in enumerate(mass_parts + cell_parts):
        scalars = jnp.where(lane == at, value, scalars)
    for m in range(slides):
        pltpu.make_async_copy(spatial_ref.at[m], tg.at[half(m)], loc.at[slides + m]).wait()

    head = backward_widths[0]
    t0[q] = tg[:, 0:head]
    for p in mates:
        send(t0.at[q], t0.at[q], t0_s, t0_r.at[q], mate(p))
    sacc[...] = jnp.zeros_like(sacc)
    s1[q, 3 * slides :, :] = jnp.zeros((8 - 3 * slides, genes), F32)
    s1[q, 3 * slides : 3 * slides + 1, 0:LANES] = scalars

    def share_logits():
        for p in (mates[1], mates[2], mates[0]):
            here = ab.at[p, half(core)]
            arrived(here, a_r.at[p])
            send(here, here, a2_s, a2_r.at[p], sibling)

    def lay_probs(p, at, value):
        af[p, at, :] = value
        there = pl.ds(pl.multiple_of(p * rows + at.start, BLOCK), BLOCK)
        probs_3[there, :] = threefold(value)

    def take_probs():
        in_blocks(0, rows, lambda at: lay_probs(q, at, pq[q, at, :]))
        for p in (mates[1], mates[2], mates[0]):
            arrived(rs.at[p], r_r.at[p])
            arrived(ab.at[p, half(1 - core)], a2_r.at[p])
            rowv[1] = jnp.concatenate([rs[p].T, jnp.zeros((rows, LANES - 8), F32)], axis=1)

            def take(at):
                probs = jnp.exp(ab[p, at, :] - rowv[1, at, 0:1]) * rowv[1, at, 1:2]
                lay_probs(p, at, probs)

            in_blocks(0, rows, take)

    def transpose(part):
        @pl.loop(0, PLANE // 2)
        def _(step):
            p = part * (PLANE // 2) + step
            high, low_part = halves(af[p].T)
            for third, value in enumerate((high, high, low_part)):
                turned_3[:, pl.ds(pl.multiple_of(third * PLANE * rows + p * rows, rows), rows)] = value

    def in_blocks(start, count, body):
        @pl.loop(0, count // BLOCK)
        def _(step):
            body(pl.ds(pl.multiple_of(start + step * BLOCK, BLOCK), BLOCK))

    quarter = lines * cb

    def lay_factor(at, length, width, value):
        high, low_part = halves(value)
        for third, part in enumerate((high, low_part, high)):
            here = pl.ds(pl.multiple_of(third * length + at.start, BLOCK), BLOCK)
            factor[here, 0:width] = part

    def keep_expr(k, at, value):
        start = sum(forward_widths[:k])
        for turn in range(turns):
            origin, width = sum(backward_widths[:turn]), backward_widths[turn]
            lo, hi = max(start, origin), min(start + forward_widths[k], origin + width)
            if lo < hi:
                high, low_part = halves(value[:, lo - start : hi - start])
                for third, part in enumerate((high, low_part, high)):
                    expr_3[at, pl.ds(3 * origin + third * width + lo - origin, hi - lo)] = part

    def three_turn_cols(k):
        return pl.ds(3 * sum(backward_widths[:k]), 3 * backward_widths[k])

    def forward_product(k):
        width = forward_widths[k]

        def lay(at):
            value = bb[k][at, :]
            lay_factor(at, quarter, width, value)
            keep_expr(k, at, value)

        in_blocks(0, quarter, lay)
        if k < chunks - 1:

            @pl.loop(0, PLANE * rows // TALL)
            def _(step):
                tall = pl.ds(pl.multiple_of(step * TALL, TALL), TALL)
                cs[k][tall, :] = product(probs_3[tall, :], factor[0 : 3 * quarter, 0:width], ((1,), (0,)))

            for p in mates:
                pass_pred(k, p)
        else:
            for side, served in ((1 - row, (mates[0], mates[2])), (row, (mates[1],))):
                pair = pl.ds(pl.multiple_of(2 * side * rows, 2 * rows), 2 * rows)
                cs[k][pair, :] = product(probs_3[pair, :], factor[0 : 3 * quarter, 0:width], ((1,), (0,)))
                for p in served:
                    pass_pred(k, p)

    def pass_pred(k, p):
        send(cs[k].at[share(p)], cr[k].at[q], c_s.at[k], c_r.at[k, q], mate(p))

    def finish_pred(k):
        total = cs[k][share(q), :]
        for p in mates:
            arrived(cr[k].at[p], c_r.at[k, p])
            total = total + cr[k][p]
        pr[:, cols(k)] = total
        if k == 0:
            p0[q] = total[:, 0:head]
            for p in mates:
                send(p0.at[q], p0.at[q], p0_s, p0_r.at[q], mate(p))
        truth = tg[:, cols(k)]
        for at, value in enumerate((total * truth, total * total, truth * truth)):
            sacc[at] += lane_groups(value)
        kept = valid * total
        stats = by_slide(kept * truth) + by_slide(kept * total) + by_slide(valid * truth * truth)
        s1[q, 0 : 3 * slides, cols(k)] = jnp.concatenate(stats, axis=0)

    early = sum(forward_widths[:EARLY])
    parts = (pl.ds(0, early), pl.ds(early, genes - early))

    def sum_plane(at):
        for p in mates:
            send(s1.at[q, :, parts[at]], s1.at[q, :, parts[at]], s1_s, s1_r.at[at, q], mate(p))

    def sum_line(at):
        for p in mates:
            arrived(s1.at[p, :, parts[at]], s1_r.at[at, p])
        s2[z, :, parts[at]] = (s1[0, :, parts[at]] + s1[1, :, parts[at]]) + (s1[2, :, parts[at]] + s1[3, :, parts[at]])
        for o in others:
            send(s2.at[z, :, parts[at]], s2.at[z, :, parts[at]], s2_s, s2_r.at[at, z], (o * PLANE + q, core))

    kept = {}

    def finish_genes(at):
        for o in others:
            arrived(s2.at[o, :, parts[at]], s2_r.at[at, o])
        total = s2[0, :, parts[at]]
        for line in range(1, lines):
            total = total + s2[line, :, parts[at]]
        gene_dot, gene_pred, gene_true = total[0:2], total[2:4], total[4:6]
        gene_inv = lax.rsqrt(gene_pred * gene_true + tiny)
        cos_gene = gene_dot * gene_inv
        gv[0:2, parts[at]] = gene_inv
        gv[2:4, parts[at]] = cos_gene * gene_true / (gene_pred * gene_true + tiny)
        kept["genes", at] = jnp.sum(jnp.sum(cos_gene, axis=1, keepdims=True), axis=0, keepdims=True)
        if at == 0:
            kept["mass"] = jnp.where(first, total[6:7, 0:1], total[6:7, 1:2])
            kept["cells"] = jnp.where(first, total[6:7, 2:3], total[6:7, 3:4])

    def sum_cores():
        sums = [jnp.sum(sacc[at], axis=1, keepdims=True) for at in range(3)]
        ss[core] = jnp.where(wide == 0, sums[0], jnp.where(wide == 1, sums[1], sums[2])).T[0:8]
        send(ss.at[core], ss.at[core], ss_s, ss_r, sibling)

    def finish_spots():
        lane_id = lax.broadcasted_iota(jnp.int32, (1, rows), 1)
        first_lane = lane_id < slide_rows
        lane_position = place * slide_rows + jnp.where(first_lane, lane_id, lane_id - slide_rows)
        lane_valid = (lane_position < jnp.where(first_lane, count_ref[0], count_ref[1])).astype(F32)
        arrived(ss.at[1 - core], ss_r)
        spot = ss[0] + ss[1]
        spot_dot, spot_pred, spot_true = spot[0:1], spot[1:2], spot[2:3]
        spot_inv = lax.rsqrt(spot_pred * spot_true + tiny)
        cos_spot = spot_dot * spot_inv
        spot_back = cos_spot * spot_true / (spot_pred * spot_true + tiny)
        kept["cos"] = jnp.sum(lane_valid * cos_spot, axis=1, keepdims=True)
        vectors = [lane_valid * spot_inv, lane_valid * spot_back, lane_valid, jnp.zeros((5, rows), F32)]
        vr[q] = jnp.concatenate(vectors, axis=0)
        sacc[0] = jnp.zeros_like(sacc[0])

    def gradient(truth, guess, by_row, k):
        pieces = []
        for m in range(slides):
            lo, hi = m * slide_rows, (m + 1) * slide_rows
            inverse, back = gv[m : m + 1, turn_cols(k)], gv[2 + m : 3 + m, turn_cols(k)]
            spot_inv, spot_back, spot_valid = by_row[lo:hi, 0:1], by_row[lo:hi, 1:2], by_row[lo:hi, 2:3]
            pieces.append(
                guess[lo:hi] * (spot_valid * back + spot_back) - truth[lo:hi] * (spot_valid * inverse + spot_inv)
            )
        return jnp.concatenate(pieces, axis=0)

    def head_gradient():
        for p in mates:
            arrived(t0.at[p], t0_r.at[p])
            arrived(p0.at[p], p0_r.at[p])
            arrived(vr.at[p], vr_r.at[p])
        for p in range(PLANE):
            ds[0][share(p), :] = gradient(t0[p], p0[p], vr[p].T, 0)
        sacc[0] += lane_groups(ds[0][share(q), :] * p0[q])

    def send_grad(k):
        if k == 0:
            for p in mates:
                send(vr.at[q], vr.at[q], vr_s, vr_r.at[q], mate(p))
            kept["by_row"] = vr[q].T
            return
        grad = gradient(tg[:, turn_cols(k)], pr[:, turn_cols(k)], kept["by_row"], k)
        here = ds[k].at[share(q)]
        here[...] = grad
        for p in mates:
            send(here, here, d_s.at[k], d_r.at[k, q], mate(p))
        sacc[0] += lane_groups(grad * pr[:, turn_cols(k)])

    def send_terms():
        mass_total, cell_total = kept["mass"], kept["cells"]
        portion = kcell / cell_total
        kl_rows = portion * (jnp.log(counted) - jnp.log(cell_total) - jnp.log(mass) + jnp.log(mass_total))
        dmass = scale_count * valid * (1.0 / mass_total - portion / mass)
        terms = jnp.sum(scale_count * kl_rows, axis=0, keepdims=True) - kept["cos"]
        l1[q] = jnp.broadcast_to(terms, (8, LANES))
        for p in mates:
            send(l1.at[q], l1.at[q], l1_s, l1_r.at[q], mate(p))
        inner = jnp.sum(sacc[0], axis=1, keepdims=True)
        inn[core] = jnp.where(wide == 0, inner, kept["genes", 0] + kept["genes", 1])
        send(inn.at[core], inn.at[core], in_s, in_r, sibling)
        rowv[1] = jnp.broadcast_to(dmass, (rows, LANES))

    middle = lines // 2

    def backward_product(k):
        if k == 0:
            head_gradient()
        else:
            for p in mates:
                arrived(ds[k].at[share(p)], d_r.at[k, p])
        width, spots = backward_widths[k], PLANE * rows

        def lay(at):
            value = ds[k][at, :]
            lay_factor(at, spots, width, value)
            grad_3[at, three_turn_cols(k)] = threefold(value)

        in_blocks(0, spots, lay)
        if not halved(k):

            @pl.loop(0, quarter // TALL)
            def _(step):
                tall = pl.ds(pl.multiple_of(step * TALL, TALL), TALL)
                es[k][tall, :] = product(turned_3[tall, :], factor[0 : 3 * spots, 0:width], ((1,), (0,)))

        for turn in range(2):
            if halved(k):
                side = (1 - z // middle) if turn == 0 else z // middle
                pair = pl.ds(pl.multiple_of(side * middle * cb, middle * cb), middle * cb)
                es[k][pair, :] = product(turned_3[pair, :], factor[0 : 3 * spots, 0:width], ((1,), (0,)))

            @pl.when(z == 0)
            def _():
                if halved(k):
                    pass_up(k, middle if turn == 0 else 1, middle if turn == 0 else middle - 1, turn)
                elif whole(k):
                    if turn == 0:
                        pass_up(k, 1, last, 0)
                elif turn == 0:
                    for line in range(last, 0, -1):
                        pass_up(k, line, 1, line)

            @pl.when(z == last)
            def _():
                if halved(k):
                    pass_down(k, 0 if turn == 0 else middle, middle if turn == 0 else middle - 1, turn)
                elif whole(k):
                    if turn == 0:
                        pass_down(k, 0, last, 0)
                elif turn == 0:
                    for line in range(last):
                        pass_down(k, line, 1, line)

    def halved(k):
        return k == 0

    def whole(k):
        return 0 < k < turns - SPLIT

    def pass_up(k, line, count, slot):
        here = pl.ds(line * cb, count * cb)
        send(es[k].at[here], ru[k].at[here], ru_s.at[k], ru_r.at[k, slot], up)

    def pass_down(k, line, count, slot):
        here = pl.ds(line * cb, count * cb)
        send(es[k].at[here], rd[k].at[here], rd_s.at[k], rd_r.at[k, slot], down)

    def take_up(k, line, count, slot):
        arrived(ru[k].at[pl.ds(line * cb, count * cb)], ru_r.at[k, slot])

    def take_down(k, line, count, slot):
        arrived(rd[k].at[pl.ds(line * cb, count * cb)], rd_r.at[k, slot])

    def add_up(k, line, count):
        def add(at):
            es[k][at, :] += ru[k][at, :]

        in_blocks(line * cb, count * cb, add)

    def add_down(k, line, count):
        def add(at):
            es[k][at, :] += rd[k][at, :]

        in_blocks(line * cb, count * cb, add)

    def rising(k, at):
        if halved(k) or whole(k):
            start = middle if halved(k) else at
            take_up(k, start, lines - start, 0)
            above = max(at + 1, start)
            add_up(k, above, lines - above)
            pass_up(k, above, lines - above, 0)
        else:
            for line in range(last, at, -1):
                take_up(k, line, 1, line)
                add_up(k, line, 1)
                pass_up(k, line, 1, line)

    def falling(k, at):
        if halved(k) or whole(k):
            end = middle if halved(k) else at + 1
            take_down(k, 0, end, 0)
            below = min(at, end)
            add_down(k, 0, below)
            pass_down(k, 0, below, 0)
        else:
            for line in range(at):
                take_down(k, line, 1, line)
                add_down(k, line, 1)
                pass_down(k, line, 1, line)

    def add_near(k):
        for at in range(1, last):

            @pl.when(z == at)
            def _():
                (rising if low(at) else falling)(k, at)

    def add_far(k):
        for at in range(1, last):

            @pl.when(z == at)
            def _():
                (falling if low(at) else rising)(k, at)

    def finish_expr(k):
        for at in range(lines):

            @pl.when(z == at)
            def _():
                if at > 0:
                    if halved(k) and at < middle:
                        take_up(k, at, 1, 1)
                    elif at == last and (halved(k) or whole(k)):
                        take_up(k, at, 1, 0)
                    elif not halved(k) and not whole(k):
                        take_up(k, at, 1, at)
                if at < last:
                    if halved(k) and at >= middle:
                        take_down(k, at, 1, 1)
                    elif at == 0 and (halved(k) or whole(k)):
                        take_down(k, at, 1, 0)
                    elif not halved(k) and not whole(k):
                        take_down(k, at, 1, at)

        from_low, from_high = z > 0, z < last

        @pl.loop(0, cb // BLOCK)
        def _(step):
            here = pl.ds(pl.multiple_of(step * BLOCK, BLOCK), BLOCK)
            own = pl.ds(pl.multiple_of(z * cb + step * BLOCK, BLOCK), BLOCK)
            total = es[k][own, :]
            total = total + jnp.where(from_low, ru[k][own, :], 0.0)
            ge[here, turn_cols(k)] = total + jnp.where(from_high, rd[k][own, :], 0.0)

    def probs_gradient(k):
        at = three_turn_cols(k)

        @pl.loop(0, PLANE * rows // TALL)
        def _(step):
            tall = pl.ds(pl.multiple_of(step * TALL, TALL), TALL)
            part = product(grad_3[tall, at], expr_3[:, at], ((1,), (1,)))
            if k == 0:
                fs[tall, :] = part
            else:
                fs[tall, :] += part

    def slide_of(p, m):
        return pl.ds(pl.multiple_of(p * rows + m * slide_rows, slide_rows), slide_rows)

    def sum_probs_cores():
        for p in mates + (q,):
            fx[p] = fs[slide_of(p, 1 - core), :]
            send(fx.at[p], fy.at[p], fx_s, fx_r.at[p], sibling)

    def return_probs():
        for p in mates:
            arrived(fy.at[p], fx_r.at[p])
            fz[p] = fs[slide_of(p, core), :] + fy[p]
            send(fz.at[p], fr.at[q], f_s, f_r.at[q], mate(p))
        arrived(fy.at[q], fx_r.at[q])
        fr[q] = fs[slide_of(q, core), :] + fy[q]

    def pass_terms():
        for p in mates:
            arrived(l1.at[p], l1_r.at[p])
        l2[z] = (l1[0] + l1[1]) + (l1[2] + l1[3])
        for o in others:
            send(l2.at[z], l2.at[z], l2_s, l2_r.at[z], (o * PLANE + q, core))

    def part_of(slide, m):
        start = slide * slide_rows + m * (slide_rows // 2)
        return pl.ds(pl.multiple_of(start, slide_rows // 2), slide_rows // 2)

    def finish_logits():
        arrived(inn.at[1 - core], in_r)
        rowv[2] = (inn[0] + inn[1]) + rowv[1] * rowv[0]
        for p in mates:
            arrived(fr.at[p], f_r.at[p])
        for m in range(2):

            @pl.loop(0, slide_rows // STEP_ROWS // 2)
            def _(step):
                row_at = (m * (slide_rows // STEP_ROWS // 2) + step) * STEP_ROWS
                at = pl.ds(pl.multiple_of(row_at, STEP_ROWS), STEP_ROWS)
                whole_at = pl.ds(pl.multiple_of(core * slide_rows + row_at, STEP_ROWS), STEP_ROWS)
                by_mass, total_inner = rowv[1, whole_at, 0:1], rowv[2, whole_at, 0:1]
                for p in range(PLANE):
                    for line in range(lines):
                        here, there = pl.ds(line * cb, cb), (line * PLANE + p) * cb
                        grad = fr[p, at, here] + by_mass * weights[:, there : there + cb]
                        glog[whole_at, pl.ds(there, cb)] = pq[p, whole_at, here] * (grad - total_inner)

            here = part_of(core, m)
            send(glog.at[here], glog.at[here], go_s, go_r.at[m], sibling)

    def forward_left():
        for k in range(chunks):

            @pl.when(z < last)
            def _():
                sent(bb[k].at[block(z)], ou_s.at[k])

            @pl.when(z > 0)
            def _():
                sent(bb[k].at[block(z)], od_s.at[k])

            for at in range(1, last):

                @pl.when(z == at)
                def _():
                    sent(bb[k].at[pl.ds(0, at * cb)], fu_s.at[k])
                    sent(bb[k].at[pl.ds((at + 1) * cb, (last - at) * cb)], fd_s.at[k])

        three = pl.ds(0, len(mates))
        sent(ab.at[three, half(0)], a_s)
        sent(ab.at[three, half(0)], a2_s)
        sent(rs.at[three], r_s)
        sent(t0.at[three], t0_s)
        sent(p0.at[three], p0_s)
        for k in range(chunks):
            sent(cr[k].at[three], c_s.at[k])
        sent(s1.at[three], s1_s)
        sent(s2.at[pl.ds(0, last)], s2_s)
        sent(ss.at[0], ss_s)

    steps = {
        "far": forward_far,
        "near": forward_near,
        "share": share_logits,
        "take": take_probs,
        "whole": gathered,
        "product": forward_product,
        "sum": finish_pred,
        "turn": transpose,
        "plane": sum_plane,
        "line": sum_line,
        "genes": finish_genes,
        "cores": sum_cores,
        "spots": finish_spots,
        "grad": send_grad,
        "terms": send_terms,
        "backward": backward_product,
        "probs": probs_gradient,
        "exchange": sum_probs_cores,
        "return": return_probs,
        "loss": pass_terms,
        "logits": finish_logits,
        "add_near": add_near,
        "add_far": add_far,
        "expr": finish_expr,
        "left": forward_left,
    }
    for name, *where in STEPS:
        steps[name](*where)

    for o in others:
        arrived(l2.at[o], l2_r.at[o])
    loss = l2[0]
    for line in range(1, lines):
        loss = loss + l2[line]
    loss_ref[...] = loss[0:1, 0:1] - (inn[0, 0:1, 1:2] + inn[1, 0:1, 1:2])
    for m in range(2):
        arrived(glog.at[part_of(1 - core, m)], go_r.at[m])

    for k in range(turns):
        for at in range(lines):

            @pl.when(z == at)
            def _():
                if at < last:
                    sent(es[k].at[pl.ds((at + 1) * cb, (last - at) * cb)], ru_s.at[k])
                if at > 0:
                    sent(es[k].at[pl.ds(0, at * cb)], rd_s.at[k])

    three = pl.ds(0, len(mates))
    for k in range(1, turns):
        sent(ds[k].at[pl.ds(0, len(mates) * rows)], d_s.at[k])
    sent(vr.at[three], vr_s)
    sent(inn.at[0], in_s)
    sent(l1.at[three], l1_s)
    sent(l2.at[pl.ds(0, last)], l2_s)
    sent(fr.at[three], f_s)
    sent(fx, fx_s)
    sent(glog.at[half(0)], go_s)


def lane_groups(value):
    parts = [value[:, at : at + LANES] for at in range(0, value.shape[1], LANES)]
    return functools.reduce(lambda a, b: a + b, parts)


def grouped(refs, sizes):
    at = 0
    for size in sizes:
        yield refs[at : at + size]
        at += size


def deliver(pred_in, loss_in, glog_in, gexp_in, pred_ref, loss_ref, glog_ref, gexp_ref, sems):
    slides, slide_rows = pred_ref.shape[0], pred_ref.shape[1]
    pairs = [(gexp_in, gexp_ref), (loss_in, loss_ref)]
    for m in range(slides):
        part = pl.ds(m * slide_rows, slide_rows)
        pairs += [(glog_in.at[part], glog_ref.at[m]), (pred_in.at[part], pred_ref.at[m])]
    copies = [pltpu.make_async_copy(src, dst, sems.at[at]) for at, (src, dst) in enumerate(pairs)]
    for copy in copies:
        copy.start()
    for copy in copies:
        copy.wait()


def plane_call(logits, expr, spatial, slide_spots, spot_cells, cell_prior, lines):
    slides, slide_rows, cells = logits.shape
    rows = slides * slide_rows
    cb, genes = expr.shape
    quarter = lines * cb
    spots = PLANE * rows
    chunks, turns = len(FORWARD), len(BACKWARD)
    dma = pltpu.SemaphoreType.DMA
    vmem = pltpu.VMEM
    anywhere = pl.BlockSpec(memory_space=pl.ANY)
    in_vmem = pl.BlockSpec(memory_space=pltpu.VMEM)
    scratch = [
        pltpu.SMEM((slides,), jnp.int32),
        vmem((slides, slide_rows), jnp.int32),
        vmem((1, cells), jnp.int32),
        vmem((rows, cells), F32),
        vmem((PLANE, slide_rows, quarter), F32),
        vmem((rows, genes), F32),
        vmem((cb, genes), F32),
        vmem((PLANE, rows, quarter), F32),
        vmem((PLANE, rows, quarter), F32),
        vmem((PLANE, rows, quarter), F32),
        vmem((spots, 3 * quarter), BF16),
        vmem((quarter, 3 * spots), BF16),
        vmem((quarter, 3 * genes), BF16),
        vmem((3, rows, LANES), F32),
        vmem((PLANE, 8, genes), F32),
        vmem((lines, 8, genes), F32),
        vmem((8, genes), F32),
        vmem((2, 8, rows), F32),
        vmem((3, rows, LANES), F32),
        vmem((PLANE, 8, rows), F32),
        vmem((spots, 3 * genes), BF16),
        vmem((3 * max(quarter, spots), max(FORWARD + BACKWARD)), BF16),
        vmem((PLANE, rows, BACKWARD[0]), F32),
        vmem((PLANE, rows, BACKWARD[0]), F32),
        vmem((PLANE, 8, rows), F32),
        vmem((spots, quarter), F32),
        vmem((PLANE, slide_rows, quarter), F32),
        vmem((PLANE, slide_rows, quarter), F32),
        vmem((PLANE, slide_rows, quarter), F32),
        vmem((PLANE, slide_rows, quarter), F32),
        vmem((2, rows, LANES), F32),
        vmem((PLANE, 8, LANES), F32),
        vmem((lines, 8, LANES), F32),
        dma((2 * slides + 4,)),
        dma((chunks,)),
        dma((chunks,)),
        dma((chunks,)),
        dma((chunks,)),
        dma((chunks,)),
        dma((chunks,)),
        dma((chunks,)),
        dma((chunks,)),
        dma,
        dma((PLANE,)),
        dma,
        dma((PLANE,)),
        dma,
        dma((PLANE,)),
        dma((chunks,)),
        dma((chunks, PLANE)),
        dma,
        dma((2, PLANE)),
        dma,
        dma((2, lines)),
        dma,
        dma,
        dma((turns,)),
        dma((turns, PLANE)),
        dma((turns,)),
        dma((turns, lines)),
        dma((turns,)),
        dma((turns, lines)),
        dma,
        dma((PLANE,)),
        dma,
        dma((PLANE,)),
        dma,
        dma((2,)),
        dma,
        dma,
        dma,
        dma((PLANE,)),
        dma,
        dma((lines,)),
        dma,
        dma((PLANE,)),
        dma,
        dma((PLANE,)),
        dma,
        dma((PLANE,)),
    ]
    for shape, widths in (
        ((quarter,), FORWARD),
        ((spots,), FORWARD),
        ((PLANE, rows), FORWARD),
        ((spots,), BACKWARD),
        ((quarter,), BACKWARD),
        ((quarter,), BACKWARD),
        ((quarter,), BACKWARD),
    ):
        scratch += [vmem(shape + (width,), F32) for width in widths]
    in_hbm = functools.partial(pltpu.with_memory_space_constraint, memory_space=pltpu.HBM)
    in_place = functools.partial(pltpu.with_memory_space_constraint, memory_space=pltpu.VMEM)
    results = pl.pallas_call(
        functools.partial(plane_kernel, lines, FORWARD, BACKWARD),
        out_shape=(
            vmem((rows, genes), F32),
            vmem((1, 1), F32),
            vmem((rows, cells), F32),
            vmem((cb, genes), F32),
        ),
        in_specs=[anywhere] * 6,
        out_specs=(in_vmem,) * 4,
        scratch_shapes=scratch,
        compiler_params=pltpu.CompilerParams(
            collective_id=0, has_side_effects=True, vmem_limit_bytes=48 * 1024 * 1024
        ),
    )(*map(in_hbm, (logits, expr, spatial, slide_spots, spot_cells, cell_prior.reshape(1, cells))))
    pred, loss, grad_logits, grad_expr = pl.pallas_call(
        deliver,
        out_shape=(
            jax.ShapeDtypeStruct((slides, slide_rows, genes), F32),
            jax.ShapeDtypeStruct((1, 1), F32),
            jax.ShapeDtypeStruct((slides, slide_rows, cells), F32),
            jax.ShapeDtypeStruct((cb, genes), F32),
        ),
        in_specs=[anywhere] * 4,
        out_specs=(anywhere,) * 4,
        scratch_shapes=[dma((2 * slides + 2,))],
        compiler_params=pltpu.CompilerParams(vmem_limit_bytes=4 * 1024 * 1024),
    )(*map(in_place, results))
    return pred, loss.reshape(()), grad_logits, grad_expr


def general_plan(logits, expr, spatial, slide_spots, spot_cells, cell_prior):
    place = lax.axis_index("spot")
    side = lax.axis_index("gene")
    rows_all = logits.shape[1]
    cell_rows = expr.shape[0]
    weights = cell_prior.astype(jnp.float32) / fixed_point
    gene_share = (place == 0).astype(jnp.float32)
    row_share = (side == 0).astype(jnp.float32)
    own_weights = lax.dynamic_slice_in_dim(weights, place * cell_rows, cell_rows, 0)
    expr_acc = jnp.zeros((cell_rows, expr.shape[1]), jnp.float32)
    loss_local = jnp.zeros((), jnp.float32)
    pred_list = []
    grad_list = []
    for slide in range(logits.shape[0]):
        logit_rows = logits[slide]
        counted = spot_cells[slide].astype(jnp.float32)
        target = spatial[slide]
        positions = place * rows_all + jnp.arange(rows_all, dtype=jnp.int32)
        valid = (positions < slide_spots[slide]).astype(jnp.float32)
        peak = jnp.max(logit_rows, axis=1, keepdims=True)
        raised = jnp.exp(logit_rows - peak)
        probs = raised / jnp.sum(raised, axis=1, keepdims=True)
        mass = jnp.dot(probs, weights, precision=lax.Precision.HIGHEST)
        blocks = lax.all_to_all(probs, "spot", split_axis=1, concat_axis=0, tiled=True)
        pred = lax.psum_scatter(
            jnp.dot(blocks, expr, precision=lax.Precision.HIGHEST),
            "spot",
            scatter_dimension=0,
            tiled=True,
        )
        gene_dot = jnp.sum(valid[:, None] * pred * target, axis=0)
        gene_pred = jnp.sum(valid[:, None] * pred * pred, axis=0)
        gene_true = jnp.sum(valid[:, None] * target * target, axis=0)
        mass_part = jnp.sum(valid * mass)
        kcell = valid * counted
        cell_part = jnp.sum(kcell)
        spot_dot = jnp.sum(pred * target, axis=1)
        spot_pred = jnp.sum(pred * pred, axis=1)
        spot_true = jnp.sum(target * target, axis=1)
        gene_dot, gene_pred, gene_true, mass_total, cell_total = lax.psum(
            (gene_dot, gene_pred, gene_true, mass_part, cell_part), "spot"
        )
        spot_dot, spot_pred, spot_true = lax.psum((spot_dot, spot_pred, spot_true), "gene")
        gene_inv = lax.rsqrt(gene_pred * gene_true + tiny)
        cos_gene = gene_dot * gene_inv
        spot_inv = lax.rsqrt(spot_pred * spot_true + tiny)
        cos_spot = spot_dot * spot_inv
        share = kcell / cell_total
        scale_count = slide_spots[slide].astype(jnp.float32)
        kl_part = jnp.sum(
            share * (jnp.log(counted) - jnp.log(cell_total) - jnp.log(mass) + jnp.log(mass_total))
        )
        loss_local = loss_local - gene_share * jnp.sum(cos_gene)
        loss_local = loss_local + row_share * (scale_count * kl_part - jnp.sum(valid * cos_spot))
        gene_back = cos_gene * gene_true / (gene_pred * gene_true + tiny)
        spot_back = cos_spot * spot_true / (spot_pred * spot_true + tiny)
        dpred = -valid[:, None] * (
            target * (gene_inv[None, :] + spot_inv[:, None])
            - pred * gene_back[None, :]
            - pred * spot_back[:, None]
        )
        dmass = scale_count * valid * (1.0 / mass_total - share / mass)
        pred_list.append(pred)
        grads_full, mass_full = (
            lax.all_gather(dpred, "spot", axis=0, tiled=True),
            lax.all_gather(dmass, "spot", axis=0, tiled=True),
        )
        dprob_cells = jnp.dot(grads_full, expr.T, precision=lax.Precision.HIGHEST)
        dprob_cells = lax.psum(dprob_cells, "gene")
        expr_acc = expr_acc + lax.dot_general(
            blocks, grads_full, (((0,), (0,)), ((), ())), precision=lax.Precision.HIGHEST
        )
        dprob_cells = dprob_cells + mass_full[:, None] * own_weights[None, :]
        dprob_rows = lax.all_to_all(dprob_cells, "spot", split_axis=0, concat_axis=1, tiled=True)
        inner = jnp.sum(probs * dprob_rows, axis=1, keepdims=True)
        dlogit = probs * (dprob_rows - inner)
        grad_list.append(dlogit)
    loss = lax.psum(loss_local, ("spot", "gene"))
    return (jnp.stack(pred_list), loss, jnp.stack(grad_list), expr_acc)


def solution(mesh):
    places = mesh.shape["spot"]

    def on_device(logits, expr, spatial, slide_spots, spot_cells, cell_prior):
        if places == PLANE * PLANE and mesh.shape["gene"] == 2 and expr.shape[1] == sum(FORWARD):
            return plane_call(
                logits, expr, spatial, slide_spots, spot_cells, cell_prior, places // PLANE
            )
        return general_plan(logits, expr, spatial, slide_spots, spot_cells, cell_prior)

    in_specs = (
        P(None, "spot", None),
        P("spot", "gene"),
        P(None, "spot", "gene"),
        P(),
        P(None, "spot"),
        P(),
    )
    out_specs = (P(None, "spot", "gene"), P(), P(None, "spot", None), P("spot", "gene"))
    return jax.shard_map(
        on_device, mesh=mesh, in_specs=in_specs, out_specs=out_specs, check_vma=False
    )
```

```python
import functools

import jax
import jax.numpy as jnp
from jax import lax
from jax.experimental import pallas as pl
from jax.experimental.pallas import tpu as pltpu
from jax.sharding import PartitionSpec as P

tiny = 1e-06
fixed_point = 16384.0
F32 = jnp.float32
BF16 = jnp.bfloat16
MESH = pl.DeviceIdType.MESH

PLANE = 4
LANES = 128
STEP_ROWS = 16
BLOCK = 32
TALL = 256
FORWARD = (128, 256, 256, 128, 128, 128)
BACKWARD = (128, 128, 256, 256, 256)
SPLIT = 4
LEAD = 1
NEAR_LEAD = 2
EARLY = 3
STEPS = (
    ("far", 0),
    ("far", 1),
    ("near", 0),
    ("share",),
    ("far", 2),
    ("far", 3),
    ("take",),
    ("whole", 0),
    ("near", 1),
    ("product", 0),
    ("sum", 0),
    ("whole", 1),
    ("near", 2),
    ("product", 1),
    ("whole", 2),
    ("product", 2),
    ("whole", 3),
    ("near", 3),
    ("product", 3),
    ("far", 4),
    ("whole", 4),
    ("near", 4),
    ("product", 4),
    ("sum", 1),
    ("turn", 0),
    ("far", 5),
    ("whole", 5),
    ("near", 5),
    ("product", 5),
    ("sum", 2),
    ("plane", 0),
    ("turn", 1),
    ("sum", 3),
    ("line", 0),
    ("sum", 4),
    ("sum", 5),
    ("plane", 1),
    ("cores",),
    ("genes", 0),
    ("spots",),
    ("grad", 0),
    ("grad", 1),
    ("grad", 2),
    ("line", 1),
    ("backward", 0),
    ("backward", 1),
    ("add_near", 0),
    ("genes", 1),
    ("grad", 3),
    ("backward", 2),
    ("probs", 0),
    ("add_far", 0),
    ("probs", 1),
    ("expr", 0),
    ("grad", 4),
    ("add_near", 1),
    ("probs", 2),
    ("terms",),
    ("backward", 3),
    ("probs", 3),
    ("add_near", 2),
    ("backward", 4),
    ("add_far", 1),
    ("probs", 4),
    ("exchange",),
    ("add_near", 3),
    ("add_far", 2),
    ("left",),
    ("return",),
    ("loss",),
    ("add_far", 3),
    ("expr", 1),
    ("add_near", 4),
    ("logits",),
    ("add_far", 4),
    ("expr", 2),
    ("expr", 3),
    ("expr", 4),
)


def halves(value):
    high = value.astype(BF16)
    return high, (value - high.astype(F32)).astype(BF16)


def threefold(value):
    high, low = halves(value)
    return jnp.concatenate([high, high, low], axis=1)


def product(a, b, contract):
    return lax.dot_general(a, b, (contract, ((), ())), preferred_element_type=F32)


def plane_kernel(lines, forward_widths, backward_widths, *refs):
    chunks, turns = len(forward_widths), len(backward_widths)
    (
        (logits_ref, expr_ref, spatial_ref, count_in, cells_in, prior_in),
        (pr, loss_ref, glog, ge),
        (count_ref, cells_ref, prior_ref, lg, lq, tg, ex, pq, ab, af, probs_3, turned_3, expr_3, sacc, s1, s2, gv, ss, rowv, rs),
        (grad_3, factor, t0, p0, vr, fs, fx, fy, fz, fr, inn, l1, l2),
        (loc, ou_s, ou_r, od_s, od_r, fu_s, fu_r, fd_s, fd_r, a_s, a_r, a2_s, a2_r, r_s, r_r),
        (c_s, c_r, s1_s, s1_r, s2_s, s2_r, ss_s, ss_r, d_s, d_r, ru_s, ru_r, rd_s, rd_r),
        (f_s, f_r, fx_s, fx_r, go_s, go_r, in_s, in_r, l1_s, l1_r, l2_s, l2_r, t0_s, t0_r, p0_s, p0_r, vr_s, vr_r),
        bb,
        cs,
        cr,
        ds,
        es,
        ru,
        rd,
    ) = grouped(refs, (6, 4, 20, 13, 15, 14, 18, chunks, chunks, chunks, turns, turns, turns, turns))
    place = lax.axis_index("spot")
    core = lax.axis_index("gene")
    z = place // PLANE
    q = place % PLANE
    col, row = q % 2, q // 2
    mates = ((1 - row) * 2 + 1 - col, row * 2 + 1 - col, (1 - row) * 2 + col)
    others = tuple((z + step) % lines for step in range(1, lines))
    up, down = (place + PLANE, core), (place - PLANE, core)
    sibling = (place, 1 - core)
    slides, slide_rows = logits_ref.shape[0], logits_ref.shape[1]
    rows = slides * slide_rows
    cb = expr_ref.shape[0]
    genes = expr_ref.shape[1]
    last = lines - 1

    def mate(p):
        return (z * PLANE + p, core)

    def send(src, dst, send_sem, recv_sem, device):
        copy = pltpu.make_async_remote_copy(
            src_ref=src, dst_ref=dst, send_sem=send_sem, recv_sem=recv_sem, device_id=device, device_id_type=MESH
        )
        copy.start()

    def arrived(dst, recv_sem):
        pltpu.make_async_copy(dst, dst, recv_sem).wait()

    sent = arrived

    def cols(k):
        return pl.ds(sum(forward_widths[:k]), forward_widths[k])

    def turn_cols(k):
        return pl.ds(sum(backward_widths[:k]), backward_widths[k])

    def block(index):
        return pl.ds(pl.multiple_of(index * cb, cb), cb)

    def share(index):
        return pl.ds(pl.multiple_of(index * rows, rows), rows)

    def half(index):
        return pl.ds(pl.multiple_of(index * slide_rows, slide_rows), slide_rows)

    small = ((prior_in, prior_ref), (count_in, count_ref), (cells_in, cells_ref))
    pltpu.make_async_copy(expr_ref, ex, loc.at[2 * slides]).start()
    for m in range(slides):
        pltpu.make_async_copy(logits_ref.at[m], lg.at[half(m)], loc.at[m]).start()
    for at, (src, dst) in enumerate(small):
        pltpu.make_async_copy(src, dst, loc.at[2 * slides + 1 + at]).start()
    for m in range(slides):
        pltpu.make_async_copy(spatial_ref.at[m], tg.at[half(m)], loc.at[slides + m]).start()

    barrier = pltpu.get_barrier_semaphore()
    for p in mates:
        pl.semaphore_signal(barrier, inc=1, device_id=mate(p), device_id_type=MESH)
    for o in others:
        pl.semaphore_signal(barrier, inc=1, device_id=(o * PLANE + q, core), device_id_type=MESH)
    pl.semaphore_signal(barrier, inc=1, device_id=sibling, device_id_type=MESH)
    pltpu.make_async_copy(expr_ref, ex, loc.at[2 * slides]).wait()
    for k in range(chunks):
        bb[k][block(z), :] = ex[:, cols(k)]
    for m in range(slides):
        pltpu.make_async_copy(logits_ref.at[m], lg.at[half(m)], loc.at[m]).wait()
    for p in range(PLANE):
        for line in range(lines):
            lq[p, :, pl.ds(line * cb, cb)] = lg[half(core), pl.ds((line * PLANE + p) * cb, cb)]
    pl.semaphore_wait(barrier, len(mates) + len(others) + 1)

    def own_up(k):
        here = bb[k].at[block(z)]
        send(here, here, ou_s.at[k], ou_r.at[k], up)

    def own_down(k):
        here = bb[k].at[block(z)]
        send(here, here, od_s.at[k], od_r.at[k], down)

    def low(at):
        return 2 * at < lines

    for at in range(lines):

        @pl.when(z == at)
        def _():
            for k in range(chunks):
                if at < last and (at == 0 or k < (LEAD if low(at) else NEAR_LEAD)):
                    own_up(k)
                if at > 0 and (at == last or k < (NEAR_LEAD if low(at) else LEAD)):
                    own_down(k)

    for p in mates:
        send(lq.at[p], ab.at[q, half(core)], a_s, a_r.at[q], mate(p))

    def from_below(k, at):
        arrived(bb[k].at[pl.ds((at - 1) * cb, cb)], ou_r.at[k])
        if at > 1:
            arrived(bb[k].at[pl.ds(0, (at - 1) * cb)], fu_r.at[k])

    def from_above(k, at):
        arrived(bb[k].at[pl.ds((at + 1) * cb, cb)], od_r.at[k])
        if at < last - 1:
            arrived(bb[k].at[pl.ds((at + 2) * cb, (last - 1 - at) * cb)], fd_r.at[k])

    def upward(k, at):
        from_below(k, at)
        here = bb[k].at[pl.ds(0, at * cb)]
        send(here, here, fu_s.at[k], fu_r.at[k], up)

    def downward(k, at):
        from_above(k, at)
        here = bb[k].at[pl.ds((at + 1) * cb, (last - at) * cb)]
        send(here, here, fd_s.at[k], fd_r.at[k], down)

    def forward_far(k):
        for at in range(1, last):

            @pl.when(z == at)
            def _():
                (upward if low(at) else downward)(k, at)
                if k + LEAD < chunks:
                    (own_up if low(at) else own_down)(k + LEAD)

    def forward_near(k):
        for at in range(1, last):

            @pl.when(z == at)
            def _():
                (downward if low(at) else upward)(k, at)
                if k + NEAR_LEAD < chunks:
                    (own_down if low(at) else own_up)(k + NEAR_LEAD)

    def gathered(k):
        @pl.when(z == 0)
        def _():
            from_above(k, 0)

        @pl.when(z == last)
        def _():
            from_below(k, last)

    for at, (src, dst) in enumerate(small):
        pltpu.make_async_copy(src, dst, loc.at[2 * slides + 1 + at]).wait()
    weights = prior_ref[...].astype(F32) / fixed_point

    @pl.loop(0, rows // STEP_ROWS)
    def _(step):
        at = pl.ds(pl.multiple_of(step * STEP_ROWS, STEP_ROWS), STEP_ROWS)
        value = lg[at, :]
        peak = jnp.max(value, axis=1, keepdims=True)
        raised = jnp.exp(value - peak)
        scale = 1.0 / jnp.sum(raised, axis=1, keepdims=True)
        probs = raised * scale
        mass_rows = jnp.sum(probs * weights, axis=1, keepdims=True)
        rowv[0, at, :] = jnp.broadcast_to(mass_rows, (STEP_ROWS, LANES))
        rowv[1, at, :] = jnp.broadcast_to(peak, (STEP_ROWS, LANES))
        rowv[2, at, :] = jnp.broadcast_to(scale, (STEP_ROWS, LANES))
        for p in range(PLANE):
            for line in range(lines):
                at_cells = (line * PLANE + p) * cb
                pq[p, at, pl.ds(line * cb, cb)] = probs[:, at_cells : at_cells + cb]

    wide = lax.broadcasted_iota(jnp.int32, (rows, LANES), 1)
    rs[q] = jnp.where(wide == 0, rowv[1], rowv[2]).T[0:8]
    for p in mates:
        send(rs.at[q], rs.at[q], r_s, r_r.at[q], mate(p))

    rid = lax.broadcasted_iota(jnp.int32, (rows, 1), 0)
    first = rid < slide_rows
    position = place * slide_rows + jnp.where(first, rid, rid - slide_rows)
    count = jnp.where(first, count_ref[0], count_ref[1])
    valid = (position < count).astype(F32)
    scale_count = count.astype(F32)
    square = (slide_rows, slide_rows)
    eye = lax.broadcasted_iota(jnp.int32, square, 0) == lax.broadcasted_iota(jnp.int32, square, 1)
    counted = jnp.concatenate(
        [
            jnp.sum(jnp.where(eye, cells_ref[m : m + 1, :].astype(F32), 0.0), axis=1, keepdims=True)
            for m in range(slides)
        ],
        axis=0,
    )
    mass = rowv[0, :, 0:1]
    kcell = valid * counted

    def by_slide(value):
        return [jnp.sum(value[m * slide_rows : (m + 1) * slide_rows], axis=0, keepdims=True) for m in range(slides)]

    mass_parts = by_slide(valid * mass)
    cell_parts = by_slide(kcell)
    lane = lax.broadcasted_iota(jnp.int32, (1, LANES), 1)
    scalars = jnp.zeros((1, LANES), F32)
    for at, value in enumerate(mass_parts + cell_parts):
        scalars = jnp.where(lane == at, value, scalars)
    for m in range(slides):
        pltpu.make_async_copy(spatial_ref.at[m], tg.at[half(m)], loc.at[slides + m]).wait()

    head = backward_widths[0]
    t0[q] = tg[:, 0:head]
    for p in mates:
        send(t0.at[q], t0.at[q], t0_s, t0_r.at[q], mate(p))
    sacc[...] = jnp.zeros_like(sacc)
    s1[q, 3 * slides :, :] = jnp.zeros((8 - 3 * slides, genes), F32)
    s1[q, 3 * slides : 3 * slides + 1, 0:LANES] = scalars

    def share_logits():
        for p in (mates[1], mates[2], mates[0]):
            here = ab.at[p, half(core)]
            arrived(here, a_r.at[p])
            send(here, here, a2_s, a2_r.at[p], sibling)

    def lay_probs(p, at, value):
        af[p, at, :] = value
        there = pl.ds(pl.multiple_of(p * rows + at.start, BLOCK), BLOCK)
        probs_3[there, :] = threefold(value)

    def take_probs():
        in_blocks(0, rows, lambda at: lay_probs(q, at, pq[q, at, :]))
        for p in (mates[1], mates[2], mates[0]):
            arrived(rs.at[p], r_r.at[p])
            arrived(ab.at[p, half(1 - core)], a2_r.at[p])
            rowv[1] = jnp.concatenate([rs[p].T, jnp.zeros((rows, LANES - 8), F32)], axis=1)

            def take(at):
                probs = jnp.exp(ab[p, at, :] - rowv[1, at, 0:1]) * rowv[1, at, 1:2]
                lay_probs(p, at, probs)

            in_blocks(0, rows, take)

    def transpose(part):
        @pl.loop(0, PLANE // 2)
        def _(step):
            p = part * (PLANE // 2) + step
            high, low_part = halves(af[p].T)
            for third, value in enumerate((high, high, low_part)):
                turned_3[:, pl.ds(pl.multiple_of(third * PLANE * rows + p * rows, rows), rows)] = value

    def in_blocks(start, count, body):
        @pl.loop(0, count // BLOCK)
        def _(step):
            body(pl.ds(pl.multiple_of(start + step * BLOCK, BLOCK), BLOCK))

    quarter = lines * cb

    def lay_factor(at, length, width, value):
        high, low_part = halves(value)
        for third, part in enumerate((high, low_part, high)):
            here = pl.ds(pl.multiple_of(third * length + at.start, BLOCK), BLOCK)
            factor[here, 0:width] = part

    def keep_expr(k, at, value):
        start = sum(forward_widths[:k])
        for turn in range(turns):
            origin, width = sum(backward_widths[:turn]), backward_widths[turn]
            lo, hi = max(start, origin), min(start + forward_widths[k], origin + width)
            if lo < hi:
                high, low_part = halves(value[:, lo - start : hi - start])
                for third, part in enumerate((high, low_part, high)):
                    expr_3[at, pl.ds(3 * origin + third * width + lo - origin, hi - lo)] = part

    def three_turn_cols(k):
        return pl.ds(3 * sum(backward_widths[:k]), 3 * backward_widths[k])

    def forward_product(k):
        width = forward_widths[k]

        def lay(at):
            value = bb[k][at, :]
            lay_factor(at, quarter, width, value)
            keep_expr(k, at, value)

        in_blocks(0, quarter, lay)
        if k < chunks - 1:

            @pl.loop(0, PLANE * rows // TALL)
            def _(step):
                tall = pl.ds(pl.multiple_of(step * TALL, TALL), TALL)
                cs[k][tall, :] = product(probs_3[tall, :], factor[0 : 3 * quarter, 0:width], ((1,), (0,)))

            for p in mates:
                pass_pred(k, p)
        else:
            for side, served in ((1 - row, (mates[0], mates[2])), (row, (mates[1],))):
                pair = pl.ds(pl.multiple_of(2 * side * rows, 2 * rows), 2 * rows)
                cs[k][pair, :] = product(probs_3[pair, :], factor[0 : 3 * quarter, 0:width], ((1,), (0,)))
                for p in served:
                    pass_pred(k, p)

    def pass_pred(k, p):
        send(cs[k].at[share(p)], cr[k].at[q], c_s.at[k], c_r.at[k, q], mate(p))

    def finish_pred(k):
        total = cs[k][share(q), :]
        for p in mates:
            arrived(cr[k].at[p], c_r.at[k, p])
            total = total + cr[k][p]
        pr[:, cols(k)] = total
        if k == 0:
            p0[q] = total[:, 0:head]
            for p in mates:
                send(p0.at[q], p0.at[q], p0_s, p0_r.at[q], mate(p))
        truth = tg[:, cols(k)]
        for at, value in enumerate((total * truth, total * total, truth * truth)):
            sacc[at] += lane_groups(value)
        kept = valid * total
        stats = by_slide(kept * truth) + by_slide(kept * total) + by_slide(valid * truth * truth)
        s1[q, 0 : 3 * slides, cols(k)] = jnp.concatenate(stats, axis=0)

    early = sum(forward_widths[:EARLY])
    parts = (pl.ds(0, early), pl.ds(early, genes - early))

    def sum_plane(at):
        for p in mates:
            send(s1.at[q, :, parts[at]], s1.at[q, :, parts[at]], s1_s, s1_r.at[at, q], mate(p))

    def sum_line(at):
        for p in mates:
            arrived(s1.at[p, :, parts[at]], s1_r.at[at, p])
        s2[z, :, parts[at]] = (s1[0, :, parts[at]] + s1[1, :, parts[at]]) + (s1[2, :, parts[at]] + s1[3, :, parts[at]])
        for o in others:
            send(s2.at[z, :, parts[at]], s2.at[z, :, parts[at]], s2_s, s2_r.at[at, z], (o * PLANE + q, core))

    kept = {}

    def finish_genes(at):
        for o in others:
            arrived(s2.at[o, :, parts[at]], s2_r.at[at, o])
        total = s2[0, :, parts[at]]
        for line in range(1, lines):
            total = total + s2[line, :, parts[at]]
        gene_dot, gene_pred, gene_true = total[0:2], total[2:4], total[4:6]
        gene_inv = lax.rsqrt(gene_pred * gene_true + tiny)
        cos_gene = gene_dot * gene_inv
        gv[0:2, parts[at]] = gene_inv
        gv[2:4, parts[at]] = cos_gene * gene_true / (gene_pred * gene_true + tiny)
        kept["genes", at] = jnp.sum(jnp.sum(cos_gene, axis=1, keepdims=True), axis=0, keepdims=True)
        if at == 0:
            kept["mass"] = jnp.where(first, total[6:7, 0:1], total[6:7, 1:2])
            kept["cells"] = jnp.where(first, total[6:7, 2:3], total[6:7, 3:4])

    def sum_cores():
        sums = [jnp.sum(sacc[at], axis=1, keepdims=True) for at in range(3)]
        ss[core] = jnp.where(wide == 0, sums[0], jnp.where(wide == 1, sums[1], sums[2])).T[0:8]
        send(ss.at[core], ss.at[core], ss_s, ss_r, sibling)

    def finish_spots():
        lane_id = lax.broadcasted_iota(jnp.int32, (1, rows), 1)
        first_lane = lane_id < slide_rows
        lane_position = place * slide_rows + jnp.where(first_lane, lane_id, lane_id - slide_rows)
        lane_valid = (lane_position < jnp.where(first_lane, count_ref[0], count_ref[1])).astype(F32)
        arrived(ss.at[1 - core], ss_r)
        spot = ss[0] + ss[1]
        spot_dot, spot_pred, spot_true = spot[0:1], spot[1:2], spot[2:3]
        spot_inv = lax.rsqrt(spot_pred * spot_true + tiny)
        cos_spot = spot_dot * spot_inv
        spot_back = cos_spot * spot_true / (spot_pred * spot_true + tiny)
        kept["cos"] = jnp.sum(lane_valid * cos_spot, axis=1, keepdims=True)
        vectors = [lane_valid * spot_inv, lane_valid * spot_back, lane_valid, jnp.zeros((5, rows), F32)]
        vr[q] = jnp.concatenate(vectors, axis=0)
        sacc[0] = jnp.zeros_like(sacc[0])

    def gradient(truth, guess, by_row, k):
        pieces = []
        for m in range(slides):
            lo, hi = m * slide_rows, (m + 1) * slide_rows
            inverse, back = gv[m : m + 1, turn_cols(k)], gv[2 + m : 3 + m, turn_cols(k)]
            spot_inv, spot_back, spot_valid = by_row[lo:hi, 0:1], by_row[lo:hi, 1:2], by_row[lo:hi, 2:3]
            pieces.append(
                guess[lo:hi] * (spot_valid * back + spot_back) - truth[lo:hi] * (spot_valid * inverse + spot_inv)
            )
        return jnp.concatenate(pieces, axis=0)

    def head_gradient():
        for p in mates:
            arrived(t0.at[p], t0_r.at[p])
            arrived(p0.at[p], p0_r.at[p])
            arrived(vr.at[p], vr_r.at[p])
        for p in range(PLANE):
            ds[0][share(p), :] = gradient(t0[p], p0[p], vr[p].T, 0)
        sacc[0] += lane_groups(ds[0][share(q), :] * p0[q])

    def send_grad(k):
        if k == 0:
            for p in mates:
                send(vr.at[q], vr.at[q], vr_s, vr_r.at[q], mate(p))
            kept["by_row"] = vr[q].T
            return
        grad = gradient(tg[:, turn_cols(k)], pr[:, turn_cols(k)], kept["by_row"], k)
        here = ds[k].at[share(q)]
        here[...] = grad
        for p in mates:
            send(here, here, d_s.at[k], d_r.at[k, q], mate(p))
        sacc[0] += lane_groups(grad * pr[:, turn_cols(k)])

    def send_terms():
        mass_total, cell_total = kept["mass"], kept["cells"]
        portion = kcell / cell_total
        kl_rows = portion * (jnp.log(counted) - jnp.log(cell_total) - jnp.log(mass) + jnp.log(mass_total))
        dmass = scale_count * valid * (1.0 / mass_total - portion / mass)
        terms = jnp.sum(scale_count * kl_rows, axis=0, keepdims=True) - kept["cos"]
        l1[q] = jnp.broadcast_to(terms, (8, LANES))
        for p in mates:
            send(l1.at[q], l1.at[q], l1_s, l1_r.at[q], mate(p))
        inner = jnp.sum(sacc[0], axis=1, keepdims=True)
        inn[core] = jnp.where(wide == 0, inner, kept["genes", 0] + kept["genes", 1])
        send(inn.at[core], inn.at[core], in_s, in_r, sibling)
        rowv[1] = jnp.broadcast_to(dmass, (rows, LANES))

    middle = lines // 2

    def backward_product(k):
        if k == 0:
            head_gradient()
        else:
            for p in mates:
                arrived(ds[k].at[share(p)], d_r.at[k, p])
        width, spots = backward_widths[k], PLANE * rows

        def lay(at):
            value = ds[k][at, :]
            lay_factor(at, spots, width, value)
            grad_3[at, three_turn_cols(k)] = threefold(value)

        in_blocks(0, spots, lay)
        if not halved(k):

            @pl.loop(0, quarter // TALL)
            def _(step):
                tall = pl.ds(pl.multiple_of(step * TALL, TALL), TALL)
                es[k][tall, :] = product(turned_3[tall, :], factor[0 : 3 * spots, 0:width], ((1,), (0,)))

        for turn in range(2):
            if halved(k):
                side = (1 - z // middle) if turn == 0 else z // middle
                pair = pl.ds(pl.multiple_of(side * middle * cb, middle * cb), middle * cb)
                es[k][pair, :] = product(turned_3[pair, :], factor[0 : 3 * spots, 0:width], ((1,), (0,)))

            @pl.when(z == 0)
            def _():
                if halved(k):
                    for line in range(last, middle - 1, -1) if turn == 0 else range(middle - 1, 0, -1):
                        pass_up(k, line, 1, line)
                elif whole(k):
                    if turn == 0:
                        pass_up(k, 1, last, 0)
                elif turn == 0:
                    for line in range(last, 0, -1):
                        pass_up(k, line, 1, line)

            @pl.when(z == last)
            def _():
                if halved(k):
                    for line in range(middle) if turn == 0 else range(middle, last):
                        pass_down(k, line, 1, line)
                elif whole(k):
                    if turn == 0:
                        pass_down(k, 0, last, 0)
                elif turn == 0:
                    for line in range(last):
                        pass_down(k, line, 1, line)

    def halved(k):
        return k == 0

    def whole(k):
        return 0 < k < turns - SPLIT

    def pass_up(k, line, count, slot):
        here = pl.ds(line * cb, count * cb)
        send(es[k].at[here], ru[k].at[here], ru_s.at[k], ru_r.at[k, slot], up)

    def pass_down(k, line, count, slot):
        here = pl.ds(line * cb, count * cb)
        send(es[k].at[here], rd[k].at[here], rd_s.at[k], rd_r.at[k, slot], down)

    def take_up(k, line, count, slot):
        arrived(ru[k].at[pl.ds(line * cb, count * cb)], ru_r.at[k, slot])

    def take_down(k, line, count, slot):
        arrived(rd[k].at[pl.ds(line * cb, count * cb)], rd_r.at[k, slot])

    def add_up(k, line, count):
        def add(at):
            es[k][at, :] += ru[k][at, :]

        in_blocks(line * cb, count * cb, add)

    def add_down(k, line, count):
        def add(at):
            es[k][at, :] += rd[k][at, :]

        in_blocks(line * cb, count * cb, add)

    def rising(k, at):
        if whole(k):
            start = at
            take_up(k, start, lines - start, 0)
            above = max(at + 1, start)
            add_up(k, above, lines - above)
            pass_up(k, above, lines - above, 0)
        else:
            for line in range(last, at, -1):
                take_up(k, line, 1, line)
                add_up(k, line, 1)
                pass_up(k, line, 1, line)

    def falling(k, at):
        if whole(k):
            end = at + 1
            take_down(k, 0, end, 0)
            below = min(at, end)
            add_down(k, 0, below)
            pass_down(k, 0, below, 0)
        else:
            for line in range(at):
                take_down(k, line, 1, line)
                add_down(k, line, 1)
                pass_down(k, line, 1, line)

    def add_near(k):
        for at in range(1, last):

            @pl.when(z == at)
            def _():
                (rising if low(at) else falling)(k, at)

    def add_far(k):
        for at in range(1, last):

            @pl.when(z == at)
            def _():
                (falling if low(at) else rising)(k, at)

    def finish_expr(k):
        for at in range(lines):

            @pl.when(z == at)
            def _():
                if at > 0:
                    if at == last and whole(k):
                        take_up(k, at, 1, 0)
                    elif not whole(k):
                        take_up(k, at, 1, at)
                if at < last:
                    if at == 0 and whole(k):
                        take_down(k, at, 1, 0)
                    elif not whole(k):
                        take_down(k, at, 1, at)

        from_low, from_high = z > 0, z < last

        @pl.loop(0, cb // BLOCK)
        def _(step):
            here = pl.ds(pl.multiple_of(step * BLOCK, BLOCK), BLOCK)
            own = pl.ds(pl.multiple_of(z * cb + step * BLOCK, BLOCK), BLOCK)
            total = es[k][own, :]
            total = total + jnp.where(from_low, ru[k][own, :], 0.0)
            ge[here, turn_cols(k)] = total + jnp.where(from_high, rd[k][own, :], 0.0)

    def probs_gradient(k):
        at = three_turn_cols(k)

        @pl.loop(0, PLANE * rows // TALL)
        def _(step):
            tall = pl.ds(pl.multiple_of(step * TALL, TALL), TALL)
            part = product(grad_3[tall, at], expr_3[:, at], ((1,), (1,)))
            if k == 0:
                fs[tall, :] = part
            else:
                fs[tall, :] += part

    def slide_of(p, m):
        return pl.ds(pl.multiple_of(p * rows + m * slide_rows, slide_rows), slide_rows)

    def sum_probs_cores():
        for p in mates + (q,):
            fx[p] = fs[slide_of(p, 1 - core), :]
            send(fx.at[p], fy.at[p], fx_s, fx_r.at[p], sibling)

    def return_probs():
        for p in mates:
            arrived(fy.at[p], fx_r.at[p])
            fz[p] = fs[slide_of(p, core), :] + fy[p]
            send(fz.at[p], fr.at[q], f_s, f_r.at[q], mate(p))
        arrived(fy.at[q], fx_r.at[q])
        fr[q] = fs[slide_of(q, core), :] + fy[q]

    def pass_terms():
        for p in mates:
            arrived(l1.at[p], l1_r.at[p])
        l2[z] = (l1[0] + l1[1]) + (l1[2] + l1[3])
        for o in others:
            send(l2.at[z], l2.at[z], l2_s, l2_r.at[z], (o * PLANE + q, core))

    def part_of(slide, m):
        start = slide * slide_rows + m * (slide_rows // 2)
        return pl.ds(pl.multiple_of(start, slide_rows // 2), slide_rows // 2)

    def finish_logits():
        arrived(inn.at[1 - core], in_r)
        rowv[2] = (inn[0] + inn[1]) + rowv[1] * rowv[0]
        for p in mates:
            arrived(fr.at[p], f_r.at[p])
        for m in range(2):

            @pl.loop(0, slide_rows // STEP_ROWS // 2)
            def _(step):
                row_at = (m * (slide_rows // STEP_ROWS // 2) + step) * STEP_ROWS
                at = pl.ds(pl.multiple_of(row_at, STEP_ROWS), STEP_ROWS)
                whole_at = pl.ds(pl.multiple_of(core * slide_rows + row_at, STEP_ROWS), STEP_ROWS)
                by_mass, total_inner = rowv[1, whole_at, 0:1], rowv[2, whole_at, 0:1]
                for p in range(PLANE):
                    for line in range(lines):
                        here, there = pl.ds(line * cb, cb), (line * PLANE + p) * cb
                        grad = fr[p, at, here] + by_mass * weights[:, there : there + cb]
                        glog[whole_at, pl.ds(there, cb)] = pq[p, whole_at, here] * (grad - total_inner)

            here = part_of(core, m)
            send(glog.at[here], glog.at[here], go_s, go_r.at[m], sibling)

    def forward_left():
        for k in range(chunks):

            @pl.when(z < last)
            def _():
                sent(bb[k].at[block(z)], ou_s.at[k])

            @pl.when(z > 0)
            def _():
                sent(bb[k].at[block(z)], od_s.at[k])

            for at in range(1, last):

                @pl.when(z == at)
                def _():
                    sent(bb[k].at[pl.ds(0, at * cb)], fu_s.at[k])
                    sent(bb[k].at[pl.ds((at + 1) * cb, (last - at) * cb)], fd_s.at[k])

        three = pl.ds(0, len(mates))
        sent(ab.at[three, half(0)], a_s)
        sent(ab.at[three, half(0)], a2_s)
        sent(rs.at[three], r_s)
        sent(t0.at[three], t0_s)
        sent(p0.at[three], p0_s)
        for k in range(chunks):
            sent(cr[k].at[three], c_s.at[k])
        sent(s1.at[three], s1_s)
        sent(s2.at[pl.ds(0, last)], s2_s)
        sent(ss.at[0], ss_s)

    steps = {
        "far": forward_far,
        "near": forward_near,
        "share": share_logits,
        "take": take_probs,
        "whole": gathered,
        "product": forward_product,
        "sum": finish_pred,
        "turn": transpose,
        "plane": sum_plane,
        "line": sum_line,
        "genes": finish_genes,
        "cores": sum_cores,
        "spots": finish_spots,
        "grad": send_grad,
        "terms": send_terms,
        "backward": backward_product,
        "probs": probs_gradient,
        "exchange": sum_probs_cores,
        "return": return_probs,
        "loss": pass_terms,
        "logits": finish_logits,
        "add_near": add_near,
        "add_far": add_far,
        "expr": finish_expr,
        "left": forward_left,
    }
    for name, *where in STEPS:
        steps[name](*where)

    for o in others:
        arrived(l2.at[o], l2_r.at[o])
    loss = l2[0]
    for line in range(1, lines):
        loss = loss + l2[line]
    loss_ref[...] = loss[0:1, 0:1] - (inn[0, 0:1, 1:2] + inn[1, 0:1, 1:2])
    for m in range(2):
        arrived(glog.at[part_of(1 - core, m)], go_r.at[m])

    for k in range(turns):
        for at in range(lines):

            @pl.when(z == at)
            def _():
                if at < last:
                    sent(es[k].at[pl.ds((at + 1) * cb, (last - at) * cb)], ru_s.at[k])
                if at > 0:
                    sent(es[k].at[pl.ds(0, at * cb)], rd_s.at[k])

    three = pl.ds(0, len(mates))
    for k in range(1, turns):
        sent(ds[k].at[pl.ds(0, len(mates) * rows)], d_s.at[k])
    sent(vr.at[three], vr_s)
    sent(inn.at[0], in_s)
    sent(l1.at[three], l1_s)
    sent(l2.at[pl.ds(0, last)], l2_s)
    sent(fr.at[three], f_s)
    sent(fx, fx_s)
    sent(glog.at[half(0)], go_s)


def lane_groups(value):
    parts = [value[:, at : at + LANES] for at in range(0, value.shape[1], LANES)]
    return functools.reduce(lambda a, b: a + b, parts)


def grouped(refs, sizes):
    at = 0
    for size in sizes:
        yield refs[at : at + size]
        at += size


def deliver(pred_in, loss_in, glog_in, gexp_in, pred_ref, loss_ref, glog_ref, gexp_ref, sems):
    slides, slide_rows = pred_ref.shape[0], pred_ref.shape[1]
    pairs = [(gexp_in, gexp_ref), (loss_in, loss_ref)]
    for m in range(slides):
        part = pl.ds(m * slide_rows, slide_rows)
        pairs += [(glog_in.at[part], glog_ref.at[m]), (pred_in.at[part], pred_ref.at[m])]
    copies = [pltpu.make_async_copy(src, dst, sems.at[at]) for at, (src, dst) in enumerate(pairs)]
    for copy in copies:
        copy.start()
    for copy in copies:
        copy.wait()


def plane_call(logits, expr, spatial, slide_spots, spot_cells, cell_prior, lines):
    slides, slide_rows, cells = logits.shape
    rows = slides * slide_rows
    cb, genes = expr.shape
    quarter = lines * cb
    spots = PLANE * rows
    chunks, turns = len(FORWARD), len(BACKWARD)
    dma = pltpu.SemaphoreType.DMA
    vmem = pltpu.VMEM
    anywhere = pl.BlockSpec(memory_space=pl.ANY)
    in_vmem = pl.BlockSpec(memory_space=pltpu.VMEM)
    scratch = [
        pltpu.SMEM((slides,), jnp.int32),
        vmem((slides, slide_rows), jnp.int32),
        vmem((1, cells), jnp.int32),
        vmem((rows, cells), F32),
        vmem((PLANE, slide_rows, quarter), F32),
        vmem((rows, genes), F32),
        vmem((cb, genes), F32),
        vmem((PLANE, rows, quarter), F32),
        vmem((PLANE, rows, quarter), F32),
        vmem((PLANE, rows, quarter), F32),
        vmem((spots, 3 * quarter), BF16),
        vmem((quarter, 3 * spots), BF16),
        vmem((quarter, 3 * genes), BF16),
        vmem((3, rows, LANES), F32),
        vmem((PLANE, 8, genes), F32),
        vmem((lines, 8, genes), F32),
        vmem((8, genes), F32),
        vmem((2, 8, rows), F32),
        vmem((3, rows, LANES), F32),
        vmem((PLANE, 8, rows), F32),
        vmem((spots, 3 * genes), BF16),
        vmem((3 * max(quarter, spots), max(FORWARD + BACKWARD)), BF16),
        vmem((PLANE, rows, BACKWARD[0]), F32),
        vmem((PLANE, rows, BACKWARD[0]), F32),
        vmem((PLANE, 8, rows), F32),
        vmem((spots, quarter), F32),
        vmem((PLANE, slide_rows, quarter), F32),
        vmem((PLANE, slide_rows, quarter), F32),
        vmem((PLANE, slide_rows, quarter), F32),
        vmem((PLANE, slide_rows, quarter), F32),
        vmem((2, rows, LANES), F32),
        vmem((PLANE, 8, LANES), F32),
        vmem((lines, 8, LANES), F32),
        dma((2 * slides + 4,)),
        dma((chunks,)),
        dma((chunks,)),
        dma((chunks,)),
        dma((chunks,)),
        dma((chunks,)),
        dma((chunks,)),
        dma((chunks,)),
        dma((chunks,)),
        dma,
        dma((PLANE,)),
        dma,
        dma((PLANE,)),
        dma,
        dma((PLANE,)),
        dma((chunks,)),
        dma((chunks, PLANE)),
        dma,
        dma((2, PLANE)),
        dma,
        dma((2, lines)),
        dma,
        dma,
        dma((turns,)),
        dma((turns, PLANE)),
        dma((turns,)),
        dma((turns, lines)),
        dma((turns,)),
        dma((turns, lines)),
        dma,
        dma((PLANE,)),
        dma,
        dma((PLANE,)),
        dma,
        dma((2,)),
        dma,
        dma,
        dma,
        dma((PLANE,)),
        dma,
        dma((lines,)),
        dma,
        dma((PLANE,)),
        dma,
        dma((PLANE,)),
        dma,
        dma((PLANE,)),
    ]
    for shape, widths in (
        ((quarter,), FORWARD),
        ((spots,), FORWARD),
        ((PLANE, rows), FORWARD),
        ((spots,), BACKWARD),
        ((quarter,), BACKWARD),
        ((quarter,), BACKWARD),
        ((quarter,), BACKWARD),
    ):
        scratch += [vmem(shape + (width,), F32) for width in widths]
    in_hbm = functools.partial(pltpu.with_memory_space_constraint, memory_space=pltpu.HBM)
    in_place = functools.partial(pltpu.with_memory_space_constraint, memory_space=pltpu.VMEM)
    results = pl.pallas_call(
        functools.partial(plane_kernel, lines, FORWARD, BACKWARD),
        out_shape=(
            vmem((rows, genes), F32),
            vmem((1, 1), F32),
            vmem((rows, cells), F32),
            vmem((cb, genes), F32),
        ),
        in_specs=[anywhere] * 6,
        out_specs=(in_vmem,) * 4,
        scratch_shapes=scratch,
        compiler_params=pltpu.CompilerParams(
            collective_id=0, has_side_effects=True, vmem_limit_bytes=48 * 1024 * 1024
        ),
    )(*map(in_hbm, (logits, expr, spatial, slide_spots, spot_cells, cell_prior.reshape(1, cells))))
    pred, loss, grad_logits, grad_expr = pl.pallas_call(
        deliver,
        out_shape=(
            jax.ShapeDtypeStruct((slides, slide_rows, genes), F32),
            jax.ShapeDtypeStruct((1, 1), F32),
            jax.ShapeDtypeStruct((slides, slide_rows, cells), F32),
            jax.ShapeDtypeStruct((cb, genes), F32),
        ),
        in_specs=[anywhere] * 4,
        out_specs=(anywhere,) * 4,
        scratch_shapes=[dma((2 * slides + 2,))],
        compiler_params=pltpu.CompilerParams(vmem_limit_bytes=4 * 1024 * 1024),
    )(*map(in_place, results))
    return pred, loss.reshape(()), grad_logits, grad_expr


def general_plan(logits, expr, spatial, slide_spots, spot_cells, cell_prior):
    place = lax.axis_index("spot")
    side = lax.axis_index("gene")
    rows_all = logits.shape[1]
    cell_rows = expr.shape[0]
    weights = cell_prior.astype(jnp.float32) / fixed_point
    gene_share = (place == 0).astype(jnp.float32)
    row_share = (side == 0).astype(jnp.float32)
    own_weights = lax.dynamic_slice_in_dim(weights, place * cell_rows, cell_rows, 0)
    expr_acc = jnp.zeros((cell_rows, expr.shape[1]), jnp.float32)
    loss_local = jnp.zeros((), jnp.float32)
    pred_list = []
    grad_list = []
    for slide in range(logits.shape[0]):
        logit_rows = logits[slide]
        counted = spot_cells[slide].astype(jnp.float32)
        target = spatial[slide]
        positions = place * rows_all + jnp.arange(rows_all, dtype=jnp.int32)
        valid = (positions < slide_spots[slide]).astype(jnp.float32)
        peak = jnp.max(logit_rows, axis=1, keepdims=True)
        raised = jnp.exp(logit_rows - peak)
        probs = raised / jnp.sum(raised, axis=1, keepdims=True)
        mass = jnp.dot(probs, weights, precision=lax.Precision.HIGHEST)
        blocks = lax.all_to_all(probs, "spot", split_axis=1, concat_axis=0, tiled=True)
        pred = lax.psum_scatter(
            jnp.dot(blocks, expr, precision=lax.Precision.HIGHEST),
            "spot",
            scatter_dimension=0,
            tiled=True,
        )
        gene_dot = jnp.sum(valid[:, None] * pred * target, axis=0)
        gene_pred = jnp.sum(valid[:, None] * pred * pred, axis=0)
        gene_true = jnp.sum(valid[:, None] * target * target, axis=0)
        mass_part = jnp.sum(valid * mass)
        kcell = valid * counted
        cell_part = jnp.sum(kcell)
        spot_dot = jnp.sum(pred * target, axis=1)
        spot_pred = jnp.sum(pred * pred, axis=1)
        spot_true = jnp.sum(target * target, axis=1)
        gene_dot, gene_pred, gene_true, mass_total, cell_total = lax.psum(
            (gene_dot, gene_pred, gene_true, mass_part, cell_part), "spot"
        )
        spot_dot, spot_pred, spot_true = lax.psum((spot_dot, spot_pred, spot_true), "gene")
        gene_inv = lax.rsqrt(gene_pred * gene_true + tiny)
        cos_gene = gene_dot * gene_inv
        spot_inv = lax.rsqrt(spot_pred * spot_true + tiny)
        cos_spot = spot_dot * spot_inv
        share = kcell / cell_total
        scale_count = slide_spots[slide].astype(jnp.float32)
        kl_part = jnp.sum(
            share * (jnp.log(counted) - jnp.log(cell_total) - jnp.log(mass) + jnp.log(mass_total))
        )
        loss_local = loss_local - gene_share * jnp.sum(cos_gene)
        loss_local = loss_local + row_share * (scale_count * kl_part - jnp.sum(valid * cos_spot))
        gene_back = cos_gene * gene_true / (gene_pred * gene_true + tiny)
        spot_back = cos_spot * spot_true / (spot_pred * spot_true + tiny)
        dpred = -valid[:, None] * (
            target * (gene_inv[None, :] + spot_inv[:, None])
            - pred * gene_back[None, :]
            - pred * spot_back[:, None]
        )
        dmass = scale_count * valid * (1.0 / mass_total - share / mass)
        pred_list.append(pred)
        grads_full, mass_full = (
            lax.all_gather(dpred, "spot", axis=0, tiled=True),
            lax.all_gather(dmass, "spot", axis=0, tiled=True),
        )
        dprob_cells = jnp.dot(grads_full, expr.T, precision=lax.Precision.HIGHEST)
        dprob_cells = lax.psum(dprob_cells, "gene")
        expr_acc = expr_acc + lax.dot_general(
            blocks, grads_full, (((0,), (0,)), ((), ())), precision=lax.Precision.HIGHEST
        )
        dprob_cells = dprob_cells + mass_full[:, None] * own_weights[None, :]
        dprob_rows = lax.all_to_all(dprob_cells, "spot", split_axis=0, concat_axis=1, tiled=True)
        inner = jnp.sum(probs * dprob_rows, axis=1, keepdims=True)
        dlogit = probs * (dprob_rows - inner)
        grad_list.append(dlogit)
    loss = lax.psum(loss_local, ("spot", "gene"))
    return (jnp.stack(pred_list), loss, jnp.stack(grad_list), expr_acc)


def solution(mesh):
    places = mesh.shape["spot"]

    def on_device(logits, expr, spatial, slide_spots, spot_cells, cell_prior):
        if places == PLANE * PLANE and mesh.shape["gene"] == 2 and expr.shape[1] == sum(FORWARD):
            return plane_call(
                logits, expr, spatial, slide_spots, spot_cells, cell_prior, places // PLANE
            )
        return general_plan(logits, expr, spatial, slide_spots, spot_cells, cell_prior)

    in_specs = (
        P(None, "spot", None),
        P("spot", "gene"),
        P(None, "spot", "gene"),
        P(),
        P(None, "spot"),
        P(),
    )
    out_specs = (P(None, "spot", "gene"), P(), P(None, "spot", None), P("spot", "gene"))
    return jax.shard_map(
        on_device, mesh=mesh, in_specs=in_specs, out_specs=out_specs, check_vma=False
    )
```

```python
import functools

import jax
import jax.numpy as jnp
from jax import lax
from jax.experimental import pallas as pl
from jax.experimental.pallas import tpu as pltpu
from jax.sharding import PartitionSpec as P

tiny = 1e-06
fixed_point = 16384.0
F32 = jnp.float32
BF16 = jnp.bfloat16
MESH = pl.DeviceIdType.MESH

PLANE = 4
LANES = 128
STEP_ROWS = 16
BLOCK = 32
TALL = 256
FORWARD = (128, 256, 256, 128, 128, 128)
BACKWARD = (128, 128, 256, 256, 256)
SPLIT = 4
LEAD = 1
NEAR_LEAD = 2
EARLY = 3
STEPS = (
    ("far", 0),
    ("far", 1),
    ("near", 0),
    ("share",),
    ("far", 2),
    ("far", 3),
    ("take",),
    ("whole", 0),
    ("near", 1),
    ("product", 0),
    ("sum", 0),
    ("whole", 1),
    ("near", 2),
    ("product", 1),
    ("whole", 2),
    ("product", 2),
    ("whole", 3),
    ("near", 3),
    ("product", 3),
    ("far", 4),
    ("whole", 4),
    ("near", 4),
    ("product", 4),
    ("sum", 1),
    ("turn", 0),
    ("far", 5),
    ("whole", 5),
    ("near", 5),
    ("product", 5),
    ("sum", 2),
    ("plane", 0),
    ("turn", 1),
    ("sum", 3),
    ("line", 0),
    ("sum", 4),
    ("sum", 5),
    ("cores",),
    ("plane", 1),
    ("genes", 0),
    ("spots",),
    ("grad", 0),
    ("grad", 1),
    ("grad", 2),
    ("line", 1),
    ("backward", 0),
    ("backward", 1),
    ("add_near", 0),
    ("genes", 1),
    ("grad", 3),
    ("backward", 2),
    ("probs", 0),
    ("add_far", 0),
    ("probs", 1),
    ("expr", 0),
    ("grad", 4),
    ("add_near", 1),
    ("probs", 2),
    ("terms",),
    ("backward", 3),
    ("probs", 3),
    ("add_near", 2),
    ("backward", 4),
    ("add_far", 1),
    ("probs", 4),
    ("exchange",),
    ("add_near", 3),
    ("add_far", 2),
    ("left",),
    ("return",),
    ("loss",),
    ("add_far", 3),
    ("expr", 1),
    ("add_near", 4),
    ("logits",),
    ("add_far", 4),
    ("expr", 2),
    ("expr", 3),
    ("expr", 4),
)


def halves(value):
    high = value.astype(BF16)
    return high, (value - high.astype(F32)).astype(BF16)


def threefold(value):
    high, low = halves(value)
    return jnp.concatenate([high, high, low], axis=1)


def product(a, b, contract):
    return lax.dot_general(a, b, (contract, ((), ())), preferred_element_type=F32)


def plane_kernel(lines, forward_widths, backward_widths, *refs):
    chunks, turns = len(forward_widths), len(backward_widths)
    (
        (logits_ref, expr_ref, spatial_ref, count_in, cells_in, prior_in),
        (pr, loss_ref, glog, ge),
        (count_ref, cells_ref, prior_ref, lg, lq, tg, ex, pq, ab, af, probs_3, turned_3, expr_3, sacc, s1, s2, gv, ss, rowv, rs),
        (grad_3, factor, t0, p0, vr, fs, fx, fy, fz, fr, inn, l1, l2),
        (loc, ou_s, ou_r, od_s, od_r, fu_s, fu_r, fd_s, fd_r, a_s, a_r, a2_s, a2_r, r_s, r_r),
        (c_s, c_r, s1_s, s1_r, s2_s, s2_r, ss_s, ss_r, d_s, d_r, ru_s, ru_r, rd_s, rd_r),
        (f_s, f_r, fx_s, fx_r, go_s, go_r, in_s, in_r, l1_s, l1_r, l2_s, l2_r, t0_s, t0_r, p0_s, p0_r, vr_s, vr_r),
        bb,
        cs,
        cr,
        ds,
        es,
        ru,
        rd,
    ) = grouped(refs, (6, 4, 20, 13, 15, 14, 18, chunks, chunks, chunks, turns, turns, turns, turns))
    place = lax.axis_index("spot")
    core = lax.axis_index("gene")
    z = place // PLANE
    q = place % PLANE
    col, row = q % 2, q // 2
    mates = ((1 - row) * 2 + 1 - col, row * 2 + 1 - col, (1 - row) * 2 + col)
    others = tuple((z + step) % lines for step in range(1, lines))
    up, down = (place + PLANE, core), (place - PLANE, core)
    sibling = (place, 1 - core)
    slides, slide_rows = logits_ref.shape[0], logits_ref.shape[1]
    rows = slides * slide_rows
    cb = expr_ref.shape[0]
    genes = expr_ref.shape[1]
    last = lines - 1

    def mate(p):
        return (z * PLANE + p, core)

    def send(src, dst, send_sem, recv_sem, device):
        copy = pltpu.make_async_remote_copy(
            src_ref=src, dst_ref=dst, send_sem=send_sem, recv_sem=recv_sem, device_id=device, device_id_type=MESH
        )
        copy.start()

    def arrived(dst, recv_sem):
        pltpu.make_async_copy(dst, dst, recv_sem).wait()

    sent = arrived

    def cols(k):
        return pl.ds(sum(forward_widths[:k]), forward_widths[k])

    def turn_cols(k):
        return pl.ds(sum(backward_widths[:k]), backward_widths[k])

    def block(index):
        return pl.ds(pl.multiple_of(index * cb, cb), cb)

    def share(index):
        return pl.ds(pl.multiple_of(index * rows, rows), rows)

    def half(index):
        return pl.ds(pl.multiple_of(index * slide_rows, slide_rows), slide_rows)

    small = ((prior_in, prior_ref), (count_in, count_ref), (cells_in, cells_ref))
    pltpu.make_async_copy(expr_ref, ex, loc.at[2 * slides]).start()
    for m in range(slides):
        pltpu.make_async_copy(logits_ref.at[m], lg.at[half(m)], loc.at[m]).start()
    for at, (src, dst) in enumerate(small):
        pltpu.make_async_copy(src, dst, loc.at[2 * slides + 1 + at]).start()
    for m in range(slides):
        pltpu.make_async_copy(spatial_ref.at[m], tg.at[half(m)], loc.at[slides + m]).start()

    barrier = pltpu.get_barrier_semaphore()
    for p in mates:
        pl.semaphore_signal(barrier, inc=1, device_id=mate(p), device_id_type=MESH)
    for o in others:
        pl.semaphore_signal(barrier, inc=1, device_id=(o * PLANE + q, core), device_id_type=MESH)
    pl.semaphore_signal(barrier, inc=1, device_id=sibling, device_id_type=MESH)
    pltpu.make_async_copy(expr_ref, ex, loc.at[2 * slides]).wait()
    for k in range(chunks):
        bb[k][block(z), :] = ex[:, cols(k)]
    for m in range(slides):
        pltpu.make_async_copy(logits_ref.at[m], lg.at[half(m)], loc.at[m]).wait()
    for p in range(PLANE):
        for line in range(lines):
            lq[p, :, pl.ds(line * cb, cb)] = lg[half(core), pl.ds((line * PLANE + p) * cb, cb)]
    pl.semaphore_wait(barrier, len(mates) + len(others) + 1)

    def own_up(k):
        here = bb[k].at[block(z)]
        send(here, here, ou_s.at[k], ou_r.at[k], up)

    def own_down(k):
        here = bb[k].at[block(z)]
        send(here, here, od_s.at[k], od_r.at[k], down)

    def low(at):
        return 2 * at < lines

    for at in range(lines):

        @pl.when(z == at)
        def _():
            for k in range(chunks):
                if at < last and (at == 0 or k < (LEAD if low(at) else NEAR_LEAD)):
                    own_up(k)
                if at > 0 and (at == last or k < (NEAR_LEAD if low(at) else LEAD)):
                    own_down(k)

    for p in mates:
        send(lq.at[p], ab.at[q, half(core)], a_s, a_r.at[q], mate(p))

    def from_below(k, at):
        arrived(bb[k].at[pl.ds((at - 1) * cb, cb)], ou_r.at[k])
        if at > 1:
            arrived(bb[k].at[pl.ds(0, (at - 1) * cb)], fu_r.at[k])

    def from_above(k, at):
        arrived(bb[k].at[pl.ds((at + 1) * cb, cb)], od_r.at[k])
        if at < last - 1:
            arrived(bb[k].at[pl.ds((at + 2) * cb, (last - 1 - at) * cb)], fd_r.at[k])

    def upward(k, at):
        from_below(k, at)
        here = bb[k].at[pl.ds(0, at * cb)]
        send(here, here, fu_s.at[k], fu_r.at[k], up)

    def downward(k, at):
        from_above(k, at)
        here = bb[k].at[pl.ds((at + 1) * cb, (last - at) * cb)]
        send(here, here, fd_s.at[k], fd_r.at[k], down)

    def forward_far(k):
        for at in range(1, last):

            @pl.when(z == at)
            def _():
                (upward if low(at) else downward)(k, at)
                if k + LEAD < chunks:
                    (own_up if low(at) else own_down)(k + LEAD)

    def forward_near(k):
        for at in range(1, last):

            @pl.when(z == at)
            def _():
                (downward if low(at) else upward)(k, at)
                if k + NEAR_LEAD < chunks:
                    (own_down if low(at) else own_up)(k + NEAR_LEAD)

    def gathered(k):
        @pl.when(z == 0)
        def _():
            from_above(k, 0)

        @pl.when(z == last)
        def _():
            from_below(k, last)

    for at, (src, dst) in enumerate(small):
        pltpu.make_async_copy(src, dst, loc.at[2 * slides + 1 + at]).wait()
    weights = prior_ref[...].astype(F32) / fixed_point

    @pl.loop(0, rows // STEP_ROWS)
    def _(step):
        at = pl.ds(pl.multiple_of(step * STEP_ROWS, STEP_ROWS), STEP_ROWS)
        value = lg[at, :]
        peak = jnp.max(value, axis=1, keepdims=True)
        raised = jnp.exp(value - peak)
        scale = 1.0 / jnp.sum(raised, axis=1, keepdims=True)
        probs = raised * scale
        mass_rows = jnp.sum(probs * weights, axis=1, keepdims=True)
        rowv[0, at, :] = jnp.broadcast_to(mass_rows, (STEP_ROWS, LANES))
        rowv[1, at, :] = jnp.broadcast_to(peak, (STEP_ROWS, LANES))
        rowv[2, at, :] = jnp.broadcast_to(scale, (STEP_ROWS, LANES))
        for p in range(PLANE):
            for line in range(lines):
                at_cells = (line * PLANE + p) * cb
                pq[p, at, pl.ds(line * cb, cb)] = probs[:, at_cells : at_cells + cb]

    wide = lax.broadcasted_iota(jnp.int32, (rows, LANES), 1)
    rs[q] = jnp.where(wide == 0, rowv[1], rowv[2]).T[0:8]
    for p in mates:
        send(rs.at[q], rs.at[q], r_s, r_r.at[q], mate(p))

    rid = lax.broadcasted_iota(jnp.int32, (rows, 1), 0)
    first = rid < slide_rows
    position = place * slide_rows + jnp.where(first, rid, rid - slide_rows)
    count = jnp.where(first, count_ref[0], count_ref[1])
    valid = (position < count).astype(F32)
    scale_count = count.astype(F32)
    square = (slide_rows, slide_rows)
    eye = lax.broadcasted_iota(jnp.int32, square, 0) == lax.broadcasted_iota(jnp.int32, square, 1)
    counted = jnp.concatenate(
        [
            jnp.sum(jnp.where(eye, cells_ref[m : m + 1, :].astype(F32), 0.0), axis=1, keepdims=True)
            for m in range(slides)
        ],
        axis=0,
    )
    mass = rowv[0, :, 0:1]
    kcell = valid * counted

    def by_slide(value):
        return [jnp.sum(value[m * slide_rows : (m + 1) * slide_rows], axis=0, keepdims=True) for m in range(slides)]

    mass_parts = by_slide(valid * mass)
    cell_parts = by_slide(kcell)
    lane = lax.broadcasted_iota(jnp.int32, (1, LANES), 1)
    scalars = jnp.zeros((1, LANES), F32)
    for at, value in enumerate(mass_parts + cell_parts):
        scalars = jnp.where(lane == at, value, scalars)
    for m in range(slides):
        pltpu.make_async_copy(spatial_ref.at[m], tg.at[half(m)], loc.at[slides + m]).wait()

    head = backward_widths[0]
    t0[q] = tg[:, 0:head]
    for p in mates:
        send(t0.at[q], t0.at[q], t0_s, t0_r.at[q], mate(p))
    sacc[...] = jnp.zeros_like(sacc)
    s1[q, 3 * slides :, :] = jnp.zeros((8 - 3 * slides, genes), F32)
    s1[q, 3 * slides : 3 * slides + 1, 0:LANES] = scalars

    def share_logits():
        for p in (mates[1], mates[2], mates[0]):
            here = ab.at[p, half(core)]
            arrived(here, a_r.at[p])
            send(here, here, a2_s, a2_r.at[p], sibling)

    def lay_probs(p, at, value):
        af[p, at, :] = value
        there = pl.ds(pl.multiple_of(p * rows + at.start, BLOCK), BLOCK)
        probs_3[there, :] = threefold(value)

    def take_probs():
        in_blocks(0, rows, lambda at: lay_probs(q, at, pq[q, at, :]))
        for p in (mates[1], mates[2], mates[0]):
            arrived(rs.at[p], r_r.at[p])
            arrived(ab.at[p, half(1 - core)], a2_r.at[p])
            rowv[1] = jnp.concatenate([rs[p].T, jnp.zeros((rows, LANES - 8), F32)], axis=1)

            def take(at):
                probs = jnp.exp(ab[p, at, :] - rowv[1, at, 0:1]) * rowv[1, at, 1:2]
                lay_probs(p, at, probs)

            in_blocks(0, rows, take)

    def transpose(part):
        @pl.loop(0, PLANE // 2)
        def _(step):
            p = part * (PLANE // 2) + step
            high, low_part = halves(af[p].T)
            for third, value in enumerate((high, high, low_part)):
                turned_3[:, pl.ds(pl.multiple_of(third * PLANE * rows + p * rows, rows), rows)] = value

    def in_blocks(start, count, body):
        @pl.loop(0, count // BLOCK)
        def _(step):
            body(pl.ds(pl.multiple_of(start + step * BLOCK, BLOCK), BLOCK))

    quarter = lines * cb

    def lay_factor(at, length, width, value):
        high, low_part = halves(value)
        for third, part in enumerate((high, low_part, high)):
            here = pl.ds(pl.multiple_of(third * length + at.start, BLOCK), BLOCK)
            factor[here, 0:width] = part

    def keep_expr(k, at, value):
        start = sum(forward_widths[:k])
        for turn in range(turns):
            origin, width = sum(backward_widths[:turn]), backward_widths[turn]
            lo, hi = max(start, origin), min(start + forward_widths[k], origin + width)
            if lo < hi:
                high, low_part = halves(value[:, lo - start : hi - start])
                for third, part in enumerate((high, low_part, high)):
                    expr_3[at, pl.ds(3 * origin + third * width + lo - origin, hi - lo)] = part

    def three_turn_cols(k):
        return pl.ds(3 * sum(backward_widths[:k]), 3 * backward_widths[k])

    def forward_product(k):
        width = forward_widths[k]

        def lay(at):
            value = bb[k][at, :]
            lay_factor(at, quarter, width, value)
            keep_expr(k, at, value)

        in_blocks(0, quarter, lay)
        if k < chunks - 1:

            @pl.loop(0, PLANE * rows // TALL)
            def _(step):
                tall = pl.ds(pl.multiple_of(step * TALL, TALL), TALL)
                cs[k][tall, :] = product(probs_3[tall, :], factor[0 : 3 * quarter, 0:width], ((1,), (0,)))

            for p in mates:
                pass_pred(k, p)
        else:
            for side, served in ((1 - row, (mates[0], mates[2])), (row, (mates[1],))):
                pair = pl.ds(pl.multiple_of(2 * side * rows, 2 * rows), 2 * rows)
                cs[k][pair, :] = product(probs_3[pair, :], factor[0 : 3 * quarter, 0:width], ((1,), (0,)))
                for p in served:
                    pass_pred(k, p)

    def pass_pred(k, p):
        send(cs[k].at[share(p)], cr[k].at[q], c_s.at[k], c_r.at[k, q], mate(p))

    def finish_pred(k):
        total = cs[k][share(q), :]
        for p in mates:
            arrived(cr[k].at[p], c_r.at[k, p])
            total = total + cr[k][p]
        pr[:, cols(k)] = total
        if k == 0:
            p0[q] = total[:, 0:head]
            for p in mates:
                send(p0.at[q], p0.at[q], p0_s, p0_r.at[q], mate(p))
        truth = tg[:, cols(k)]
        for at, value in enumerate((total * truth, total * total, truth * truth)):
            sacc[at] += lane_groups(value)
        kept = valid * total
        stats = by_slide(kept * truth) + by_slide(kept * total) + by_slide(valid * truth * truth)
        s1[q, 0 : 3 * slides, cols(k)] = jnp.concatenate(stats, axis=0)

    early = sum(forward_widths[:EARLY])
    parts = (pl.ds(0, early), pl.ds(early, genes - early))

    def sum_plane(at):
        for p in mates:
            send(s1.at[q, :, parts[at]], s1.at[q, :, parts[at]], s1_s, s1_r.at[at, q], mate(p))

    def sum_line(at):
        for p in mates:
            arrived(s1.at[p, :, parts[at]], s1_r.at[at, p])
        s2[z, :, parts[at]] = (s1[0, :, parts[at]] + s1[1, :, parts[at]]) + (s1[2, :, parts[at]] + s1[3, :, parts[at]])
        for o in others:
            send(s2.at[z, :, parts[at]], s2.at[z, :, parts[at]], s2_s, s2_r.at[at, z], (o * PLANE + q, core))

    kept = {}

    def finish_genes(at):
        for o in others:
            arrived(s2.at[o, :, parts[at]], s2_r.at[at, o])
        total = s2[0, :, parts[at]]
        for line in range(1, lines):
            total = total + s2[line, :, parts[at]]
        gene_dot, gene_pred, gene_true = total[0:2], total[2:4], total[4:6]
        gene_inv = lax.rsqrt(gene_pred * gene_true + tiny)
        cos_gene = gene_dot * gene_inv
        gv[0:2, parts[at]] = gene_inv
        gv[2:4, parts[at]] = cos_gene * gene_true / (gene_pred * gene_true + tiny)
        kept["genes", at] = jnp.sum(jnp.sum(cos_gene, axis=1, keepdims=True), axis=0, keepdims=True)
        if at == 0:
            kept["mass"] = jnp.where(first, total[6:7, 0:1], total[6:7, 1:2])
            kept["cells"] = jnp.where(first, total[6:7, 2:3], total[6:7, 3:4])

    def sum_cores():
        sums = [jnp.sum(sacc[at], axis=1, keepdims=True) for at in range(3)]
        ss[core] = jnp.where(wide == 0, sums[0], jnp.where(wide == 1, sums[1], sums[2])).T[0:8]
        send(ss.at[core], ss.at[core], ss_s, ss_r, sibling)

    def finish_spots():
        lane_id = lax.broadcasted_iota(jnp.int32, (1, rows), 1)
        first_lane = lane_id < slide_rows
        lane_position = place * slide_rows + jnp.where(first_lane, lane_id, lane_id - slide_rows)
        lane_valid = (lane_position < jnp.where(first_lane, count_ref[0], count_ref[1])).astype(F32)
        arrived(ss.at[1 - core], ss_r)
        spot = ss[0] + ss[1]
        spot_dot, spot_pred, spot_true = spot[0:1], spot[1:2], spot[2:3]
        spot_inv = lax.rsqrt(spot_pred * spot_true + tiny)
        cos_spot = spot_dot * spot_inv
        spot_back = cos_spot * spot_true / (spot_pred * spot_true + tiny)
        kept["cos"] = jnp.sum(lane_valid * cos_spot, axis=1, keepdims=True)
        vectors = [lane_valid * spot_inv, lane_valid * spot_back, lane_valid, jnp.zeros((5, rows), F32)]
        vr[q] = jnp.concatenate(vectors, axis=0)
        sacc[0] = jnp.zeros_like(sacc[0])

    def gradient(truth, guess, by_row, k):
        pieces = []
        for m in range(slides):
            lo, hi = m * slide_rows, (m + 1) * slide_rows
            inverse, back = gv[m : m + 1, turn_cols(k)], gv[2 + m : 3 + m, turn_cols(k)]
            spot_inv, spot_back, spot_valid = by_row[lo:hi, 0:1], by_row[lo:hi, 1:2], by_row[lo:hi, 2:3]
            pieces.append(
                guess[lo:hi] * (spot_valid * back + spot_back) - truth[lo:hi] * (spot_valid * inverse + spot_inv)
            )
        return jnp.concatenate(pieces, axis=0)

    def head_gradient():
        for p in mates:
            arrived(t0.at[p], t0_r.at[p])
            arrived(p0.at[p], p0_r.at[p])
            arrived(vr.at[p], vr_r.at[p])
        for p in range(PLANE):
            ds[0][share(p), :] = gradient(t0[p], p0[p], vr[p].T, 0)
        sacc[0] += lane_groups(ds[0][share(q), :] * p0[q])

    def send_grad(k):
        if k == 0:
            for p in mates:
                send(vr.at[q], vr.at[q], vr_s, vr_r.at[q], mate(p))
            kept["by_row"] = vr[q].T
            return
        grad = gradient(tg[:, turn_cols(k)], pr[:, turn_cols(k)], kept["by_row"], k)
        here = ds[k].at[share(q)]
        here[...] = grad
        for p in mates:
            send(here, here, d_s.at[k], d_r.at[k, q], mate(p))
        sacc[0] += lane_groups(grad * pr[:, turn_cols(k)])

    def send_terms():
        mass_total, cell_total = kept["mass"], kept["cells"]
        portion = kcell / cell_total
        kl_rows = portion * (jnp.log(counted) - jnp.log(cell_total) - jnp.log(mass) + jnp.log(mass_total))
        dmass = scale_count * valid * (1.0 / mass_total - portion / mass)
        terms = jnp.sum(scale_count * kl_rows, axis=0, keepdims=True) - kept["cos"]
        l1[q] = jnp.broadcast_to(terms, (8, LANES))
        for p in mates:
            send(l1.at[q], l1.at[q], l1_s, l1_r.at[q], mate(p))
        inner = jnp.sum(sacc[0], axis=1, keepdims=True)
        inn[core] = jnp.where(wide == 0, inner, kept["genes", 0] + kept["genes", 1])
        send(inn.at[core], inn.at[core], in_s, in_r, sibling)
        rowv[1] = jnp.broadcast_to(dmass, (rows, LANES))

    middle = lines // 2

    def backward_product(k):
        if k == 0:
            head_gradient()
        else:
            for p in mates:
                arrived(ds[k].at[share(p)], d_r.at[k, p])
        width, spots = backward_widths[k], PLANE * rows

        def lay(at):
            value = ds[k][at, :]
            lay_factor(at, spots, width, value)
            grad_3[at, three_turn_cols(k)] = threefold(value)

        in_blocks(0, spots, lay)
        if not halved(k):

            @pl.loop(0, quarter // TALL)
            def _(step):
                tall = pl.ds(pl.multiple_of(step * TALL, TALL), TALL)
                es[k][tall, :] = product(turned_3[tall, :], factor[0 : 3 * spots, 0:width], ((1,), (0,)))

        for turn in range(2):
            if halved(k):
                side = (1 - z // middle) if turn == 0 else z // middle
                pair = pl.ds(pl.multiple_of(side * middle * cb, middle * cb), middle * cb)
                es[k][pair, :] = product(turned_3[pair, :], factor[0 : 3 * spots, 0:width], ((1,), (0,)))

            @pl.when(z == 0)
            def _():
                if halved(k):
                    for line in range(last, middle - 1, -1) if turn == 0 else range(middle - 1, 0, -1):
                        pass_up(k, line, 1, line)
                elif whole(k):
                    if turn == 0:
                        pass_up(k, 1, last, 0)
                elif turn == 0:
                    for line in range(last, 0, -1):
                        pass_up(k, line, 1, line)

            @pl.when(z == last)
            def _():
                if halved(k):
                    for line in range(middle) if turn == 0 else range(middle, last):
                        pass_down(k, line, 1, line)
                elif whole(k):
                    if turn == 0:
                        pass_down(k, 0, last, 0)
                elif turn == 0:
                    for line in range(last):
                        pass_down(k, line, 1, line)

    def halved(k):
        return k == 0

    def whole(k):
        return 0 < k < turns - SPLIT

    def pass_up(k, line, count, slot):
        here = pl.ds(line * cb, count * cb)
        send(es[k].at[here], ru[k].at[here], ru_s.at[k], ru_r.at[k, slot], up)

    def pass_down(k, line, count, slot):
        here = pl.ds(line * cb, count * cb)
        send(es[k].at[here], rd[k].at[here], rd_s.at[k], rd_r.at[k, slot], down)

    def take_up(k, line, count, slot):
        arrived(ru[k].at[pl.ds(line * cb, count * cb)], ru_r.at[k, slot])

    def take_down(k, line, count, slot):
        arrived(rd[k].at[pl.ds(line * cb, count * cb)], rd_r.at[k, slot])

    def add_up(k, line, count):
        def add(at):
            es[k][at, :] += ru[k][at, :]

        in_blocks(line * cb, count * cb, add)

    def add_down(k, line, count):
        def add(at):
            es[k][at, :] += rd[k][at, :]

        in_blocks(line * cb, count * cb, add)

    def rising(k, at):
        if whole(k):
            start = at
            take_up(k, start, lines - start, 0)
            above = max(at + 1, start)
            add_up(k, above, lines - above)
            pass_up(k, above, lines - above, 0)
        else:
            for line in range(last, at, -1):
                take_up(k, line, 1, line)
                add_up(k, line, 1)
                pass_up(k, line, 1, line)

    def falling(k, at):
        if whole(k):
            end = at + 1
            take_down(k, 0, end, 0)
            below = min(at, end)
            add_down(k, 0, below)
            pass_down(k, 0, below, 0)
        else:
            for line in range(at):
                take_down(k, line, 1, line)
                add_down(k, line, 1)
                pass_down(k, line, 1, line)

    def add_near(k):
        for at in range(1, last):

            @pl.when(z == at)
            def _():
                (rising if low(at) else falling)(k, at)

    def add_far(k):
        for at in range(1, last):

            @pl.when(z == at)
            def _():
                (falling if low(at) else rising)(k, at)

    def finish_expr(k):
        for at in range(lines):

            @pl.when(z == at)
            def _():
                if at > 0:
                    if at == last and whole(k):
                        take_up(k, at, 1, 0)
                    elif not whole(k):
                        take_up(k, at, 1, at)
                if at < last:
                    if at == 0 and whole(k):
                        take_down(k, at, 1, 0)
                    elif not whole(k):
                        take_down(k, at, 1, at)

        from_low, from_high = z > 0, z < last

        @pl.loop(0, cb // BLOCK)
        def _(step):
            here = pl.ds(pl.multiple_of(step * BLOCK, BLOCK), BLOCK)
            own = pl.ds(pl.multiple_of(z * cb + step * BLOCK, BLOCK), BLOCK)
            total = es[k][own, :]
            total = total + jnp.where(from_low, ru[k][own, :], 0.0)
            ge[here, turn_cols(k)] = total + jnp.where(from_high, rd[k][own, :], 0.0)

    def probs_gradient(k):
        at = three_turn_cols(k)

        @pl.loop(0, PLANE * rows // TALL)
        def _(step):
            tall = pl.ds(pl.multiple_of(step * TALL, TALL), TALL)
            part = product(grad_3[tall, at], expr_3[:, at], ((1,), (1,)))
            if k == 0:
                fs[tall, :] = part
            else:
                fs[tall, :] += part

    def slide_of(p, m):
        return pl.ds(pl.multiple_of(p * rows + m * slide_rows, slide_rows), slide_rows)

    def sum_probs_cores():
        for p in mates + (q,):
            fx[p] = fs[slide_of(p, 1 - core), :]
            send(fx.at[p], fy.at[p], fx_s, fx_r.at[p], sibling)

    def return_probs():
        for p in mates:
            arrived(fy.at[p], fx_r.at[p])
            fz[p] = fs[slide_of(p, core), :] + fy[p]
            send(fz.at[p], fr.at[q], f_s, f_r.at[q], mate(p))
        arrived(fy.at[q], fx_r.at[q])
        fr[q] = fs[slide_of(q, core), :] + fy[q]

    def pass_terms():
        for p in mates:
            arrived(l1.at[p], l1_r.at[p])
        l2[z] = (l1[0] + l1[1]) + (l1[2] + l1[3])
        for o in others:
            send(l2.at[z], l2.at[z], l2_s, l2_r.at[z], (o * PLANE + q, core))

    def part_of(slide, m):
        start = slide * slide_rows + m * (slide_rows // 2)
        return pl.ds(pl.multiple_of(start, slide_rows // 2), slide_rows // 2)

    def finish_logits():
        arrived(inn.at[1 - core], in_r)
        rowv[2] = (inn[0] + inn[1]) + rowv[1] * rowv[0]
        for p in mates:
            arrived(fr.at[p], f_r.at[p])
        for m in range(2):

            @pl.loop(0, slide_rows // STEP_ROWS // 2)
            def _(step):
                row_at = (m * (slide_rows // STEP_ROWS // 2) + step) * STEP_ROWS
                at = pl.ds(pl.multiple_of(row_at, STEP_ROWS), STEP_ROWS)
                whole_at = pl.ds(pl.multiple_of(core * slide_rows + row_at, STEP_ROWS), STEP_ROWS)
                by_mass, total_inner = rowv[1, whole_at, 0:1], rowv[2, whole_at, 0:1]
                for p in range(PLANE):
                    for line in range(lines):
                        here, there = pl.ds(line * cb, cb), (line * PLANE + p) * cb
                        grad = fr[p, at, here] + by_mass * weights[:, there : there + cb]
                        glog[whole_at, pl.ds(there, cb)] = pq[p, whole_at, here] * (grad - total_inner)

            here = part_of(core, m)
            send(glog.at[here], glog.at[here], go_s, go_r.at[m], sibling)

    def forward_left():
        for k in range(chunks):

            @pl.when(z < last)
            def _():
                sent(bb[k].at[block(z)], ou_s.at[k])

            @pl.when(z > 0)
            def _():
                sent(bb[k].at[block(z)], od_s.at[k])

            for at in range(1, last):

                @pl.when(z == at)
                def _():
                    sent(bb[k].at[pl.ds(0, at * cb)], fu_s.at[k])
                    sent(bb[k].at[pl.ds((at + 1) * cb, (last - at) * cb)], fd_s.at[k])

        three = pl.ds(0, len(mates))
        sent(ab.at[three, half(0)], a_s)
        sent(ab.at[three, half(0)], a2_s)
        sent(rs.at[three], r_s)
        sent(t0.at[three], t0_s)
        sent(p0.at[three], p0_s)
        for k in range(chunks):
            sent(cr[k].at[three], c_s.at[k])
        sent(s1.at[three], s1_s)
        sent(s2.at[pl.ds(0, last)], s2_s)
        sent(ss.at[0], ss_s)

    steps = {
        "far": forward_far,
        "near": forward_near,
        "share": share_logits,
        "take": take_probs,
        "whole": gathered,
        "product": forward_product,
        "sum": finish_pred,
        "turn": transpose,
        "plane": sum_plane,
        "line": sum_line,
        "genes": finish_genes,
        "cores": sum_cores,
        "spots": finish_spots,
        "grad": send_grad,
        "terms": send_terms,
        "backward": backward_product,
        "probs": probs_gradient,
        "exchange": sum_probs_cores,
        "return": return_probs,
        "loss": pass_terms,
        "logits": finish_logits,
        "add_near": add_near,
        "add_far": add_far,
        "expr": finish_expr,
        "left": forward_left,
    }
    for name, *where in STEPS:
        steps[name](*where)

    for o in others:
        arrived(l2.at[o], l2_r.at[o])
    loss = l2[0]
    for line in range(1, lines):
        loss = loss + l2[line]
    loss_ref[...] = loss[0:1, 0:1] - (inn[0, 0:1, 1:2] + inn[1, 0:1, 1:2])
    for m in range(2):
        arrived(glog.at[part_of(1 - core, m)], go_r.at[m])

    for k in range(turns):
        for at in range(lines):

            @pl.when(z == at)
            def _():
                if at < last:
                    sent(es[k].at[pl.ds((at + 1) * cb, (last - at) * cb)], ru_s.at[k])
                if at > 0:
                    sent(es[k].at[pl.ds(0, at * cb)], rd_s.at[k])

    three = pl.ds(0, len(mates))
    for k in range(1, turns):
        sent(ds[k].at[pl.ds(0, len(mates) * rows)], d_s.at[k])
    sent(vr.at[three], vr_s)
    sent(inn.at[0], in_s)
    sent(l1.at[three], l1_s)
    sent(l2.at[pl.ds(0, last)], l2_s)
    sent(fr.at[three], f_s)
    sent(fx, fx_s)
    sent(glog.at[half(0)], go_s)


def lane_groups(value):
    parts = [value[:, at : at + LANES] for at in range(0, value.shape[1], LANES)]
    return functools.reduce(lambda a, b: a + b, parts)


def grouped(refs, sizes):
    at = 0
    for size in sizes:
        yield refs[at : at + size]
        at += size


def deliver(pred_in, loss_in, glog_in, gexp_in, pred_ref, loss_ref, glog_ref, gexp_ref, sems):
    slides, slide_rows = pred_ref.shape[0], pred_ref.shape[1]
    pairs = [(gexp_in, gexp_ref), (loss_in, loss_ref)]
    for m in range(slides):
        part = pl.ds(m * slide_rows, slide_rows)
        pairs += [(glog_in.at[part], glog_ref.at[m]), (pred_in.at[part], pred_ref.at[m])]
    copies = [pltpu.make_async_copy(src, dst, sems.at[at]) for at, (src, dst) in enumerate(pairs)]
    for copy in copies:
        copy.start()
    for copy in copies:
        copy.wait()


def plane_call(logits, expr, spatial, slide_spots, spot_cells, cell_prior, lines):
    slides, slide_rows, cells = logits.shape
    rows = slides * slide_rows
    cb, genes = expr.shape
    quarter = lines * cb
    spots = PLANE * rows
    chunks, turns = len(FORWARD), len(BACKWARD)
    dma = pltpu.SemaphoreType.DMA
    vmem = pltpu.VMEM
    anywhere = pl.BlockSpec(memory_space=pl.ANY)
    in_vmem = pl.BlockSpec(memory_space=pltpu.VMEM)
    scratch = [
        pltpu.SMEM((slides,), jnp.int32),
        vmem((slides, slide_rows), jnp.int32),
        vmem((1, cells), jnp.int32),
        vmem((rows, cells), F32),
        vmem((PLANE, slide_rows, quarter), F32),
        vmem((rows, genes), F32),
        vmem((cb, genes), F32),
        vmem((PLANE, rows, quarter), F32),
        vmem((PLANE, rows, quarter), F32),
        vmem((PLANE, rows, quarter), F32),
        vmem((spots, 3 * quarter), BF16),
        vmem((quarter, 3 * spots), BF16),
        vmem((quarter, 3 * genes), BF16),
        vmem((3, rows, LANES), F32),
        vmem((PLANE, 8, genes), F32),
        vmem((lines, 8, genes), F32),
        vmem((8, genes), F32),
        vmem((2, 8, rows), F32),
        vmem((3, rows, LANES), F32),
        vmem((PLANE, 8, rows), F32),
        vmem((spots, 3 * genes), BF16),
        vmem((3 * max(quarter, spots), max(FORWARD + BACKWARD)), BF16),
        vmem((PLANE, rows, BACKWARD[0]), F32),
        vmem((PLANE, rows, BACKWARD[0]), F32),
        vmem((PLANE, 8, rows), F32),
        vmem((spots, quarter), F32),
        vmem((PLANE, slide_rows, quarter), F32),
        vmem((PLANE, slide_rows, quarter), F32),
        vmem((PLANE, slide_rows, quarter), F32),
        vmem((PLANE, slide_rows, quarter), F32),
        vmem((2, rows, LANES), F32),
        vmem((PLANE, 8, LANES), F32),
        vmem((lines, 8, LANES), F32),
        dma((2 * slides + 4,)),
        dma((chunks,)),
        dma((chunks,)),
        dma((chunks,)),
        dma((chunks,)),
        dma((chunks,)),
        dma((chunks,)),
        dma((chunks,)),
        dma((chunks,)),
        dma,
        dma((PLANE,)),
        dma,
        dma((PLANE,)),
        dma,
        dma((PLANE,)),
        dma((chunks,)),
        dma((chunks, PLANE)),
        dma,
        dma((2, PLANE)),
        dma,
        dma((2, lines)),
        dma,
        dma,
        dma((turns,)),
        dma((turns, PLANE)),
        dma((turns,)),
        dma((turns, lines)),
        dma((turns,)),
        dma((turns, lines)),
        dma,
        dma((PLANE,)),
        dma,
        dma((PLANE,)),
        dma,
        dma((2,)),
        dma,
        dma,
        dma,
        dma((PLANE,)),
        dma,
        dma((lines,)),
        dma,
        dma((PLANE,)),
        dma,
        dma((PLANE,)),
        dma,
        dma((PLANE,)),
    ]
    for shape, widths in (
        ((quarter,), FORWARD),
        ((spots,), FORWARD),
        ((PLANE, rows), FORWARD),
        ((spots,), BACKWARD),
        ((quarter,), BACKWARD),
        ((quarter,), BACKWARD),
        ((quarter,), BACKWARD),
    ):
        scratch += [vmem(shape + (width,), F32) for width in widths]
    in_hbm = functools.partial(pltpu.with_memory_space_constraint, memory_space=pltpu.HBM)
    in_place = functools.partial(pltpu.with_memory_space_constraint, memory_space=pltpu.VMEM)
    results = pl.pallas_call(
        functools.partial(plane_kernel, lines, FORWARD, BACKWARD),
        out_shape=(
            vmem((rows, genes), F32),
            vmem((1, 1), F32),
            vmem((rows, cells), F32),
            vmem((cb, genes), F32),
        ),
        in_specs=[anywhere] * 6,
        out_specs=(in_vmem,) * 4,
        scratch_shapes=scratch,
        compiler_params=pltpu.CompilerParams(
            collective_id=0, has_side_effects=True, vmem_limit_bytes=48 * 1024 * 1024
        ),
    )(*map(in_hbm, (logits, expr, spatial, slide_spots, spot_cells, cell_prior.reshape(1, cells))))
    pred, loss, grad_logits, grad_expr = pl.pallas_call(
        deliver,
        out_shape=(
            jax.ShapeDtypeStruct((slides, slide_rows, genes), F32),
            jax.ShapeDtypeStruct((1, 1), F32),
            jax.ShapeDtypeStruct((slides, slide_rows, cells), F32),
            jax.ShapeDtypeStruct((cb, genes), F32),
        ),
        in_specs=[anywhere] * 4,
        out_specs=(anywhere,) * 4,
        scratch_shapes=[dma((2 * slides + 2,))],
        compiler_params=pltpu.CompilerParams(vmem_limit_bytes=4 * 1024 * 1024),
    )(*map(in_place, results))
    return pred, loss.reshape(()), grad_logits, grad_expr


def general_plan(logits, expr, spatial, slide_spots, spot_cells, cell_prior):
    place = lax.axis_index("spot")
    side = lax.axis_index("gene")
    rows_all = logits.shape[1]
    cell_rows = expr.shape[0]
    weights = cell_prior.astype(jnp.float32) / fixed_point
    gene_share = (place == 0).astype(jnp.float32)
    row_share = (side == 0).astype(jnp.float32)
    own_weights = lax.dynamic_slice_in_dim(weights, place * cell_rows, cell_rows, 0)
    expr_acc = jnp.zeros((cell_rows, expr.shape[1]), jnp.float32)
    loss_local = jnp.zeros((), jnp.float32)
    pred_list = []
    grad_list = []
    for slide in range(logits.shape[0]):
        logit_rows = logits[slide]
        counted = spot_cells[slide].astype(jnp.float32)
        target = spatial[slide]
        positions = place * rows_all + jnp.arange(rows_all, dtype=jnp.int32)
        valid = (positions < slide_spots[slide]).astype(jnp.float32)
        peak = jnp.max(logit_rows, axis=1, keepdims=True)
        raised = jnp.exp(logit_rows - peak)
        probs = raised / jnp.sum(raised, axis=1, keepdims=True)
        mass = jnp.dot(probs, weights, precision=lax.Precision.HIGHEST)
        blocks = lax.all_to_all(probs, "spot", split_axis=1, concat_axis=0, tiled=True)
        pred = lax.psum_scatter(
            jnp.dot(blocks, expr, precision=lax.Precision.HIGHEST),
            "spot",
            scatter_dimension=0,
            tiled=True,
        )
        gene_dot = jnp.sum(valid[:, None] * pred * target, axis=0)
        gene_pred = jnp.sum(valid[:, None] * pred * pred, axis=0)
        gene_true = jnp.sum(valid[:, None] * target * target, axis=0)
        mass_part = jnp.sum(valid * mass)
        kcell = valid * counted
        cell_part = jnp.sum(kcell)
        spot_dot = jnp.sum(pred * target, axis=1)
        spot_pred = jnp.sum(pred * pred, axis=1)
        spot_true = jnp.sum(target * target, axis=1)
        gene_dot, gene_pred, gene_true, mass_total, cell_total = lax.psum(
            (gene_dot, gene_pred, gene_true, mass_part, cell_part), "spot"
        )
        spot_dot, spot_pred, spot_true = lax.psum((spot_dot, spot_pred, spot_true), "gene")
        gene_inv = lax.rsqrt(gene_pred * gene_true + tiny)
        cos_gene = gene_dot * gene_inv
        spot_inv = lax.rsqrt(spot_pred * spot_true + tiny)
        cos_spot = spot_dot * spot_inv
        share = kcell / cell_total
        scale_count = slide_spots[slide].astype(jnp.float32)
        kl_part = jnp.sum(
            share * (jnp.log(counted) - jnp.log(cell_total) - jnp.log(mass) + jnp.log(mass_total))
        )
        loss_local = loss_local - gene_share * jnp.sum(cos_gene)
        loss_local = loss_local + row_share * (scale_count * kl_part - jnp.sum(valid * cos_spot))
        gene_back = cos_gene * gene_true / (gene_pred * gene_true + tiny)
        spot_back = cos_spot * spot_true / (spot_pred * spot_true + tiny)
        dpred = -valid[:, None] * (
            target * (gene_inv[None, :] + spot_inv[:, None])
            - pred * gene_back[None, :]
            - pred * spot_back[:, None]
        )
        dmass = scale_count * valid * (1.0 / mass_total - share / mass)
        pred_list.append(pred)
        grads_full, mass_full = (
            lax.all_gather(dpred, "spot", axis=0, tiled=True),
            lax.all_gather(dmass, "spot", axis=0, tiled=True),
        )
        dprob_cells = jnp.dot(grads_full, expr.T, precision=lax.Precision.HIGHEST)
        dprob_cells = lax.psum(dprob_cells, "gene")
        expr_acc = expr_acc + lax.dot_general(
            blocks, grads_full, (((0,), (0,)), ((), ())), precision=lax.Precision.HIGHEST
        )
        dprob_cells = dprob_cells + mass_full[:, None] * own_weights[None, :]
        dprob_rows = lax.all_to_all(dprob_cells, "spot", split_axis=0, concat_axis=1, tiled=True)
        inner = jnp.sum(probs * dprob_rows, axis=1, keepdims=True)
        dlogit = probs * (dprob_rows - inner)
        grad_list.append(dlogit)
    loss = lax.psum(loss_local, ("spot", "gene"))
    return (jnp.stack(pred_list), loss, jnp.stack(grad_list), expr_acc)


def solution(mesh):
    places = mesh.shape["spot"]

    def on_device(logits, expr, spatial, slide_spots, spot_cells, cell_prior):
        if places == PLANE * PLANE and mesh.shape["gene"] == 2 and expr.shape[1] == sum(FORWARD):
            return plane_call(
                logits, expr, spatial, slide_spots, spot_cells, cell_prior, places // PLANE
            )
        return general_plan(logits, expr, spatial, slide_spots, spot_cells, cell_prior)

    in_specs = (
        P(None, "spot", None),
        P("spot", "gene"),
        P(None, "spot", "gene"),
        P(),
        P(None, "spot"),
        P(),
    )
    out_specs = (P(None, "spot", "gene"), P(), P(None, "spot", None), P("spot", "gene"))
    return jax.shard_map(
        on_device, mesh=mesh, in_specs=in_specs, out_specs=out_specs, check_vma=False
    )
```
